32 devices in a mesh: dp: 16 (over z, x, core), mp: 2 (over y).
Axes of the slice: x: 2, y: 2, z: 4, core: 2. Of those that a mesh axis runs over, the one named last changes fastest.
Arguments:
- tokens: bfloat16 [4096, 2560], P(('dp', 'mp')), may hold values from -6 to 6
- segments: int32 [4096], P('dp'), may hold values from 0 to 3, as said below
- positions: int32 [4096], P('dp'), may hold values from 0 to 511, as said below
- cotangent: bfloat16 [4096, 2560], P(('dp', 'mp')), may hold values from -6 to 6
- attn_gain: bfloat16 [2560], P(('dp', 'mp')), may hold values from 0.25 to 1.75
- ffn_gain: bfloat16 [2560], P(('dp', 'mp')), may hold values from 0.25 to 1.75
- w_kv: bfloat16 [2560, 512], P(('dp', 'mp')), may hold values from -0.125 to 0.125
- w_query: bfloat16 [2560, 2560], P('dp', 'mp'), may hold values from -0.25 to 0.25
- w_out: bfloat16 [2560, 2560], P('dp', 'mp'), may hold values from -0.5 to 0.5
- w_gate: bfloat16 [2560, 7680], P('dp', 'mp'), may hold values from -0.125 to 0.125
- w_up: bfloat16 [2560, 7680], P('dp', 'mp'), may hold values from -0.125 to 0.125
- w_down: bfloat16 [2560, 7680], P('dp', 'mp'), may hold values from -0.0625 to 0.0625
Outputs:
- mixed: bfloat16 [4096, 2560], P(('dp', 'mp'))
- tokens_grad: bfloat16 [4096, 2560], P(('dp', 'mp'))
- attn_gain_grad: float32 [2560], P(('dp', 'mp'))
- ffn_gain_grad: float32 [2560], P(('dp', 'mp'))
- w_kv_grad: float32 [2560, 512], P(('dp', 'mp'))
- w_query_grad: float32 [2560, 2560], P('dp', 'mp')
- w_out_grad: float32 [2560, 2560], P('dp', 'mp')
- w_gate_grad: float32 [2560, 7680], P('dp', 'mp')
- w_up_grad: float32 [2560, 7680], P('dp', 'mp')
- w_down_grad: float32 [2560, 7680], P('dp', 'mp')
The draws below stay inside these ranges and needn't reach their ends.
Inputs may be any that keep to these rules, and one draw needn't show every extreme that they name: `segments`: within each sequence of 256 tokens the ids start at 0 and never fall; each id covers consecutive tokens. Inside a document positions rise by one from token to token; they start at 0 at every document that begins inside the sequence.
All inputs are finite; a program needn't handle non-finite values.
Results may differ from the reference program's by a relative error of at most 0.015.
Values may be sent and summed in bfloat16 or wider, within the bound.
A program may use at most 320 MiB of HBM per device.

```python
import jax
import jax.numpy as jnp
from jax import lax

D = 2560
HEADS = 10
HD = 256
FF = 7680
WINDOW = 2048
SEQ = 256
TOKENS = 4096
N_MP = 2


def cut_points(key):
    row_count = TOKENS // SEQ
    key_one, key_two, key_three, key_four = jax.random.split(key, 4)
    eighth = SEQ // 8
    first_cut = jax.random.randint(key_one, (row_count, 1), 1, eighth + 1)
    second_cut = first_cut + jax.random.randint(key_two, (row_count, 1), 1, eighth + 1)
    third_cut = jax.random.randint(key_three, (row_count, 1), 3 * SEQ // 4, SEQ)
    places = jnp.arange(SEQ, dtype=jnp.int32)[None, :]
    ids = (places >= first_cut).astype(jnp.int32) + (places >= second_cut).astype(jnp.int32) + (places >= third_cut).astype(jnp.int32)
    doc_start = jnp.where(places >= third_cut, third_cut, jnp.where(places >= second_cut, second_cut, jnp.where(places >= first_cut, first_cut, 0)))
    top_offset = 2 * SEQ - first_cut
    offset = jax.random.randint(key_four, (row_count, 1), 0, top_offset + 1)
    offset = offset.at[0].set(top_offset[0])
    where_first = (places < first_cut).astype(jnp.int32)
    placed = places - doc_start + where_first * offset
    return (ids.reshape(-1).astype(jnp.int32), placed.reshape(-1).astype(jnp.int32))


def draw_segments(key, part):
    shared = cut_points(key)
    return shared[0]


def draw_positions(key, part):
    shared = cut_points(key)
    return shared[1]


def raised(values, key, source, target, parts, factor):
    def block_of(position):
        return (jnp.arange(values.shape[position]) // (values.shape[position] // parts)).reshape((-1,) + (1,) * (values.ndim - 1 - position))

    first = jax.random.permutation(key, parts)[block_of(target)]
    second = (block_of(target) + parts // 2) % parts
    return jnp.where((block_of(source) == first) | (block_of(source) == second), factor * values, values)


def block_levels(rng, dims, cuts, low, top_value):
    loudness = 1.0
    for axis_at, parts in cuts:
        steps = jax.random.uniform(jax.random.fold_in(jax.random.fold_in(rng, 6), axis_at), (parts,), jnp.float32, low / len(cuts), top_value / len(cuts))
        loudness = loudness * jnp.repeat(jnp.exp(steps), dims[axis_at] // parts).reshape((-1,) + (1,) * (len(dims) - 1 - axis_at))
    return loudness


def gaussian(stream_key, shape, deviation, limit, cuts=(), kind=jnp.bfloat16):
    level = block_levels(stream_key, shape, cuts, -0.22, 0.18) if cuts else 1.0
    values = jax.random.normal(stream_key, shape, jnp.float32) * deviation * level
    return jnp.minimum(jnp.maximum(values, -limit), limit).astype(kind)


def gaussian_with(own_key, extent, spread, reach, cuts, heavy, kind=jnp.bfloat16):
    values = spread * jax.random.normal(own_key, extent, jnp.float32)
    if cuts:
        values = values * block_levels(own_key, extent, cuts, -0.22, 0.18)
    return jnp.clip(raised(values, jax.random.fold_in(own_key, 3), *heavy), -reach, reach).astype(kind)


def setup_inputs(seed: int = 0) -> dict:
    arg_keys = jax.random.split(jax.random.key(seed), 13)
    return {
        "tokens": gaussian(arg_keys[0], (TOKENS, D), 1.0, 6.0, ((0, 32),)),
        "segments": draw_segments(jax.random.fold_in(arg_keys[12], 71), 0),
        "positions": draw_positions(jax.random.fold_in(arg_keys[12], 71), 0),
        "cotangent": gaussian_with(arg_keys[3], (TOKENS, D), 1.0, 6.0, ((0, 32),), (0, 1, 32, 2.75)),
        "attn_gain": jnp.clip(1.0 + 0.15 * jax.random.normal(arg_keys[4], (D,), jnp.float32), 0.25, 1.75).astype(jnp.bfloat16),
        "ffn_gain": jnp.clip(1.0 + 0.15 * jax.random.normal(arg_keys[5], (D,), jnp.float32), 0.25, 1.75).astype(jnp.bfloat16),
        "w_kv": gaussian(arg_keys[6], (D, 2 * HD), D ** -0.5, 0.125, ((0, 32),)),
        "w_query": gaussian(arg_keys[7], (D, HEADS * HD), (D // 4) ** -0.5, 0.25, ((0, 16), (1, 2))),
        "w_out": gaussian(arg_keys[8], (D, HEADS * HD), (HEADS * HD // 16) ** -0.5, 0.5, ((0, 16), (1, 2))),
        "w_gate": gaussian(arg_keys[9], (D, FF), D ** -0.5, 0.125, ((0, 16), (1, 2))),
        "w_up": gaussian(arg_keys[10], (D, FF), D ** -0.5, 0.125, ((0, 16), (1, 2))),
        "w_down": gaussian(arg_keys[11], (D, FF), FF ** -0.5, 0.0625, ((0, 16), (1, 2))),
    }


@jax.custom_vjp
def low(v):
    return lax.optimization_barrier(v.astype(jnp.bfloat16)).astype(jnp.float32)

@jax.custom_vjp
def low_back(v):
    return v

def low_keep(v):
    return (low(v), None)

def low_pass(kept, grad):
    return (grad,)

def back_keep(v):
    return (v, None)

def back_low(kept, grad):
    return (low(grad),)
low.defvjp(low_keep, low_pass)
low_back.defvjp(back_keep, back_low)
epsilon = 1e-06
rope_base = 10000.0
highest = lax.Precision.HIGHEST

def exact_dot(left, right):
    return jnp.dot(left, right, precision=highest)

def norm_gain(values, gain):
    return values * lax.rsqrt(lax.optimization_barrier(jnp.mean(values * values, axis=-1, keepdims=True)) + epsilon) * gain

def rotary_angles(positions, head_width):
    quarter = head_width // 4
    freqs = rope_base ** (-jnp.arange(quarter).astype(jnp.float32) / quarter)
    phase = positions.astype(jnp.float32)[:, None] * freqs[None, :]
    return (jnp.cos(phase), jnp.sin(phase))

def rotate(values, cosine, sine):
    quarter = cosine.shape[-1]
    first_half = values[..., :quarter]
    second_half = values[..., quarter:2 * quarter]
    return jnp.concatenate([first_half * cosine - second_half * sine, second_half * cosine + first_half * sine, values[..., 2 * quarter:]], axis=-1)

def attend(queries, keys, values, allowed):
    scores = low_back(jnp.einsum('thd,sd->hts', queries, keys, precision=highest))
    scores = jnp.where(allowed[None], scores, -1e+30)
    probs = low(jax.nn.softmax(scores, axis=-1))
    return jnp.einsum('hts,sd->thd', probs, values, precision=highest)

def block_layer(tokens_row, params, segment_row, position_row):
    gain_one, gain_two, kv_weight, query_weight, out_weight, gate_weight, up_weight, down_weight = params
    seq_len = tokens_row.shape[0]
    normed_one = low(norm_gain(tokens_row, gain_one))
    query = low_back(exact_dot(normed_one, query_weight)).reshape(seq_len, HEADS, HD)
    cosine, sine = rotary_angles(position_row, HD)
    rotated = low(rotate(query, cosine[:, None], sine[:, None]) * HD ** (-0.5))
    places = jnp.arange(seq_len)
    allowed = (segment_row[:, None] == segment_row[None, :]) & (places[None, :] <= places[:, None]) & (places[:, None] - places[None, :] < WINDOW)
    per_group = HEADS // N_MP
    pieces = []
    for group in range(N_MP):
        keyval = low_back(exact_dot(normed_one, kv_weight))
        keys = low(rotate(keyval[:, :HD], cosine, sine))
        values = low(keyval[:, HD:])
        pieces.append(attend(rotated[:, group * per_group:(group + 1) * per_group], keys, values, allowed))
    attn_vals = low(low_back(jnp.concatenate(pieces, axis=1).reshape(seq_len, HEADS * HD)))
    mid = tokens_row + low_back(exact_dot(attn_vals, out_weight.T))
    normed_two = low(norm_gain(mid, gain_two))
    gate = low_back(exact_dot(normed_two, gate_weight))
    up_proj = low_back(exact_dot(normed_two, up_weight))
    hidden = low(jax.nn.gelu(gate, approximate=True) * up_proj)
    return mid + exact_dot(hidden, down_weight.T)

def reference(tokens, segments, positions, cotangent, attn_gain, ffn_gain, w_kv, w_query, w_out, w_gate, w_up, w_down):
    params = tuple((weight.astype(jnp.float32) for weight in (attn_gain, ffn_gain, w_kv, w_query, w_out, w_gate, w_up, w_down)))
    seq_count = TOKENS // SEQ
    inputs = (tokens.astype(jnp.float32).reshape(seq_count, SEQ, D), segments.reshape(seq_count, SEQ), positions.reshape(seq_count, SEQ), cotangent.astype(jnp.float32).reshape(seq_count, SEQ, D))

    def per_sequence(totals, sequence_item):
        tokens_row, segment_row, position_row, grad_row = sequence_item

        def forward_pass(inputs_row, weights):
            return block_layer(inputs_row, weights, segment_row, position_row)
        outputs_row, pullback = jax.vjp(forward_pass, tokens_row, params)
        grad_tokens, grad_params = pullback(grad_row)
        totals = jax.tree.map(jnp.add, totals, grad_params)
        return (totals, (outputs_row.astype(jnp.bfloat16), grad_tokens.astype(jnp.bfloat16)))
    zeros = tuple((jnp.zeros_like(weight) for weight in params))
    totals, outputs = lax.scan(per_sequence, zeros, inputs)
    mixed = outputs[0].reshape(TOKENS, D)
    tokens_grad = outputs[1].reshape(TOKENS, D)
    return (mixed, tokens_grad, totals[0], totals[1], totals[2], totals[3], totals[4], totals[5], totals[6], totals[7])
```

```python
import jax
import jax.numpy as jnp
from jax import lax
from jax.sharding import PartitionSpec as P

WINDOW = 2048


epsilon = 1e-06
rope_base = 10000.0
masked_score = -1e30
score_rows = 512


def norm_gain(values, gain):
    return values * lax.rsqrt(jnp.mean(values * values, axis=-1, keepdims=True) + epsilon) * gain


def rotary_angles(positions, head_width):
    quarter = head_width // 4
    freqs = rope_base ** (-jnp.arange(quarter).astype(jnp.float32) / quarter)
    phase = positions.astype(jnp.float32)[:, None] * freqs[None, :]
    return (jnp.cos(phase), jnp.sin(phase))


def rotate(values, cosine, sine):
    quarter = cosine.shape[-1]
    first_half = values[..., :quarter]
    second_half = values[..., quarter : 2 * quarter]
    return jnp.concatenate(
        [
            first_half * cosine - second_half * sine,
            second_half * cosine + first_half * sine,
            values[..., 2 * quarter :],
        ],
        axis=-1,
    )


def unrotate(values, cosine, sine):
    quarter = cosine.shape[-1]
    first_half = values[..., :quarter]
    second_half = values[..., quarter : 2 * quarter]
    return jnp.concatenate(
        [
            first_half * cosine + second_half * sine,
            second_half * cosine - first_half * sine,
            values[..., 2 * quarter :],
        ],
        axis=-1,
    )


def gelu_product(gate, up_proj):
    return jax.nn.gelu(gate, approximate=True) * up_proj


def matmul_nt(left, right):
    return lax.dot_general(
        left, right, (((1,), (1,)), ((), ())), preferred_element_type=jnp.float32
    )


def matmul_tn(left, right):
    return lax.dot_general(
        left, right, (((0,), (0,)), ((), ())), preferred_element_type=jnp.float32
    )


def block_allowed(segments, first_row, rows):
    seq_len = segments.shape[0]
    query_rows = first_row + jnp.arange(rows)
    key_rows = jnp.arange(seq_len)
    return (
        (segments[:, None] == segments[None, :])
        & (key_rows[None, :] <= query_rows[:, None])
        & (query_rows[:, None] - key_rows[None, :] < WINDOW)
    )


FF_SPLIT = 4


def ffn_pass(normed, grad_out, gate_weight, up_weight, down_weight):
    gate = jnp.dot(normed, gate_weight, preferred_element_type=jnp.float32)
    up_proj = jnp.dot(normed, up_weight, preferred_element_type=jnp.float32)
    grad_hidden = jnp.dot(grad_out, down_weight, preferred_element_type=jnp.float32)
    product, pull = jax.vjp(gelu_product, gate, up_proj)
    hidden = product.astype(jnp.bfloat16)
    grad_gate_f, grad_up_f = pull(grad_hidden)
    grad_gate = grad_gate_f.astype(jnp.bfloat16)
    grad_up = grad_up_f.astype(jnp.bfloat16)
    mixed_part = matmul_nt(hidden, down_weight).astype(jnp.bfloat16)
    normed_part = (matmul_nt(grad_gate, gate_weight) + matmul_nt(grad_up, up_weight)).astype(
        jnp.bfloat16
    )
    weight_parts = [
        matmul_tn(normed, grad_gate).astype(jnp.bfloat16),
        matmul_tn(normed, grad_up).astype(jnp.bfloat16),
        matmul_tn(grad_out, hidden).astype(jnp.bfloat16),
    ]
    return mixed_part, normed_part, weight_parts


def shards(
    tokens,
    segments,
    positions,
    cotangent,
    attn_gain,
    ffn_gain,
    w_kv,
    w_query,
    w_out,
    w_gate,
    w_up,
    w_down,
):
    everywhere = ("z", "xc", "mp")
    dp = ("z", "xc")
    z_size = lax.axis_size("z")
    xc_size = lax.axis_size("xc")
    gains = lax.all_gather(
        jnp.stack([attn_gain, ffn_gain], axis=1), everywhere, axis=0, tiled=True
    ).astype(jnp.float32)
    gain_one, gain_two = gains[:, 0], gains[:, 1]
    kv_weight = lax.all_gather(w_kv, everywhere, axis=0, tiled=True)
    head_dim = kv_weight.shape[1] // 2
    width = tokens.shape[1]
    seq_len = segments.shape[0]
    heads_here = w_query.shape[1] // head_dim
    scale = head_dim ** (-0.5)
    cosine, sine = rotary_angles(positions, head_dim)
    inputs_f = tokens.astype(jnp.float32)
    tokens_all = lax.all_gather(tokens, "mp", axis=0, tiled=True)
    normed_one = norm_gain(tokens_all.astype(jnp.float32), gain_one).astype(jnp.bfloat16)
    query_weight = lax.all_gather(w_query, dp, axis=0, tiled=True)
    out_weight = lax.all_gather(w_out, dp, axis=0, tiled=True)

    rows = w_gate.shape[0]
    unit = w_gate.shape[1] // z_size

    def spread(weight):
        pieces = weight.reshape(rows, z_size, unit).transpose(1, 0, 2)
        pieces = lax.all_to_all(pieces, "z", split_axis=0, concat_axis=0, tiled=True)
        return lax.all_gather(pieces, "xc", axis=1, tiled=False).reshape(width, unit)

    gate_weight, up_weight, down_weight = spread(w_gate), spread(w_up), spread(w_down)
    grad_all = lax.all_gather(cotangent, ("z", "mp"), axis=0, tiled=True)

    query = jnp.dot(normed_one, query_weight, preferred_element_type=jnp.float32).reshape(
        seq_len, heads_here, head_dim
    )
    rotated = (rotate(query, cosine[:, None], sine[:, None]) * scale).astype(jnp.bfloat16)
    keyval = jnp.dot(normed_one, kv_weight, preferred_element_type=jnp.float32)
    keys = rotate(keyval[:, :head_dim], cosine, sine).astype(jnp.bfloat16)
    values = keyval[:, head_dim:].astype(jnp.bfloat16)
    allowed = block_allowed(segments, 0, seq_len)
    scores = jnp.einsum("thd,sd->hts", rotated, keys, preferred_element_type=jnp.float32)
    scores = jnp.where(allowed[None], scores, masked_score)
    row_max = jnp.max(scores, axis=-1, keepdims=True)
    weights = jnp.exp(scores - row_max)
    probs = weights / jnp.sum(weights, axis=-1, keepdims=True)
    probs_low = probs.astype(jnp.bfloat16)
    attn_vals = (
        jnp.einsum("hts,sd->thd", probs_low, values, preferred_element_type=jnp.float32)
        .reshape(seq_len, heads_here * head_dim)
        .astype(jnp.bfloat16)
    )
    mid = inputs_f + lax.psum_scatter(
        matmul_nt(attn_vals, out_weight).astype(jnp.bfloat16),
        "mp",
        scatter_dimension=0,
        tiled=True,
    ).astype(jnp.float32)
    normed_two = norm_gain(mid, gain_two).astype(jnp.bfloat16)
    normed_all = lax.all_gather(normed_two, ("z", "mp"), axis=0, tiled=True)

    mixed_part, normed_part, weight_parts = ffn_pass(
        normed_all, grad_all, gate_weight, up_weight, down_weight
    )
    grad_normed_two = lax.psum_scatter(
        normed_part, ("z", "mp"), scatter_dimension=0, tiled=True
    ).astype(jnp.float32)
    mixed = (
        mid
        + lax.psum_scatter(mixed_part, ("z", "mp"), scatter_dimension=0, tiled=True).astype(
            jnp.float32
        )
    ).astype(jnp.bfloat16)

    def collect(part):
        pieces = part.reshape(z_size, xc_size, rows, unit).transpose(1, 0, 2, 3)
        pieces = pieces.reshape(xc_size * z_size * rows, unit)
        pieces = lax.psum_scatter(pieces, "xc", scatter_dimension=0, tiled=True)
        pieces = pieces.reshape(z_size, rows, unit)
        pieces = lax.all_to_all(pieces, "z", split_axis=0, concat_axis=0, tiled=True)
        return pieces.transpose(1, 0, 2).reshape(rows, z_size * unit).astype(jnp.float32)

    w_gate_grad, w_up_grad, w_down_grad = [collect(part) for part in weight_parts]

    norm_pull_two = jax.vjp(norm_gain, mid, gain_two)[1]
    grad_mid_norm, grad_gain_two = norm_pull_two(grad_normed_two)
    grad_mid = cotangent.astype(jnp.float32) + grad_mid_norm
    grad_mid_all = lax.all_gather(grad_mid.astype(jnp.bfloat16), "mp", axis=0, tiled=True)
    grad_vals = (
        jnp.dot(grad_mid_all, out_weight, preferred_element_type=jnp.float32)
        .astype(jnp.bfloat16)
        .reshape(seq_len, heads_here, head_dim)
    )
    grad_probs = jnp.einsum("thd,sd->hts", grad_vals, values, preferred_element_type=jnp.float32)
    delta = jnp.sum(probs * grad_probs, axis=-1, keepdims=True)
    grad_scores = (probs * (grad_probs - delta)).astype(jnp.bfloat16)
    grad_rot = jnp.einsum("hts,sd->thd", grad_scores, keys, preferred_element_type=jnp.float32)
    key_sum = jnp.einsum("hts,thd->sd", grad_scores, rotated, preferred_element_type=jnp.float32)
    value_sum = jnp.einsum("hts,thd->sd", probs_low, grad_vals, preferred_element_type=jnp.float32)
    grad_query = (
        (unrotate(grad_rot, cosine[:, None], sine[:, None]) * scale)
        .reshape(seq_len, heads_here * head_dim)
        .astype(jnp.bfloat16)
    )
    grad_kv = jnp.concatenate([unrotate(key_sum, cosine, sine), value_sum], axis=1).astype(
        jnp.bfloat16
    )
    grad_normed_one = lax.psum_scatter(
        (matmul_nt(grad_query, query_weight) + matmul_nt(grad_kv, kv_weight)).astype(jnp.bfloat16),
        "mp",
        scatter_dimension=0,
        tiled=True,
    ).astype(jnp.float32)
    norm_pull_one = jax.vjp(norm_gain, inputs_f, gain_one)[1]
    grad_input_norm, grad_gain_one = norm_pull_one(grad_normed_one)
    tokens_grad = (grad_mid + grad_input_norm).astype(jnp.bfloat16)

    w_query_grad = lax.psum_scatter(
        matmul_tn(normed_one, grad_query).astype(jnp.bfloat16), dp, scatter_dimension=0, tiled=True
    ).astype(jnp.float32)
    w_out_grad = lax.psum_scatter(
        matmul_tn(grad_mid_all, attn_vals).astype(jnp.bfloat16), dp, scatter_dimension=0, tiled=True
    ).astype(jnp.float32)
    small = jnp.concatenate(
        [matmul_tn(normed_one, grad_kv), grad_gain_one[:, None], grad_gain_two[:, None]], axis=1
    )
    small = lax.psum_scatter(small, everywhere, scatter_dimension=0, tiled=True)
    kv_grad = small[:, : 2 * head_dim]
    return (
        mixed,
        tokens_grad,
        small[:, 2 * head_dim],
        small[:, 2 * head_dim + 1],
        kv_grad,
        w_query_grad,
        w_out_grad,
        w_gate_grad,
        w_up_grad,
        w_down_grad,
    )


def solution(mesh):
    dp_size, mp_size = mesh.shape["dp"], mesh.shape["mp"]
    fine = jax.sharding.Mesh(
        mesh.devices.reshape(FF_SPLIT, dp_size // FF_SPLIT, mp_size), ("z", "xc", "mp")
    )
    dp = ("z", "xc")
    all_axes = ("z", "xc", "mp")
    in_specs = (
        P(all_axes, None),
        P(dp),
        P(dp),
        P(all_axes, None),
        P(all_axes),
        P(all_axes),
        P(all_axes, None),
        P(dp, "mp"),
        P(dp, "mp"),
        P(dp, "mp"),
        P(dp, "mp"),
        P(dp, "mp"),
    )
    out_specs = (
        P(all_axes, None),
        P(all_axes, None),
        P(all_axes),
        P(all_axes),
        P(all_axes, None),
        P(dp, "mp"),
        P(dp, "mp"),
        P(dp, "mp"),
        P(dp, "mp"),
        P(dp, "mp"),
    )
    return jax.shard_map(shards, mesh=fine, in_specs=in_specs, out_specs=out_specs, check_vma=False)
```

```python
import functools

import jax
import jax.numpy as jnp
from jax import lax
from jax.experimental import pallas as pl
from jax.experimental.pallas import tpu as pltpu
from jax.sharding import PartitionSpec as P

WINDOW = 2048


epsilon = 1e-06
rope_base = 10000.0
masked_score = -1e30
VMEM_BYTES = 62 * 1024 * 1024


def norm_gain(values, gain):
    return values * lax.rsqrt(jnp.mean(values * values, axis=-1, keepdims=True) + epsilon) * gain


def rotary_angles(positions, head_width):
    quarter = head_width // 4
    freqs = rope_base ** (-jnp.arange(quarter).astype(jnp.float32) / quarter)
    phase = positions.astype(jnp.float32)[:, None] * freqs[None, :]
    return (jnp.cos(phase), jnp.sin(phase))


def rotate(values, cosine, sine):
    quarter = cosine.shape[-1]
    first_half = values[..., :quarter]
    second_half = values[..., quarter : 2 * quarter]
    return jnp.concatenate(
        [
            first_half * cosine - second_half * sine,
            second_half * cosine + first_half * sine,
            values[..., 2 * quarter :],
        ],
        axis=-1,
    )


def unrotate(values, cosine, sine):
    quarter = cosine.shape[-1]
    first_half = values[..., :quarter]
    second_half = values[..., quarter : 2 * quarter]
    return jnp.concatenate(
        [
            first_half * cosine + second_half * sine,
            second_half * cosine - first_half * sine,
            values[..., 2 * quarter :],
        ],
        axis=-1,
    )


def gelu_product(gate, up_proj):
    return jax.nn.gelu(gate, approximate=True) * up_proj


def matmul_nt(left, right):
    return lax.dot_general(
        left, right, (((1,), (1,)), ((), ())), preferred_element_type=jnp.float32
    )


def matmul_tn(left, right):
    return lax.dot_general(
        left, right, (((0,), (0,)), ((), ())), preferred_element_type=jnp.float32
    )


def block_allowed(segments, first_row, rows):
    seq_len = segments.shape[0]
    query_rows = first_row + jnp.arange(rows)
    key_rows = jnp.arange(seq_len)
    return (
        (segments[:, None] == segments[None, :])
        & (key_rows[None, :] <= query_rows[:, None])
        & (query_rows[:, None] - key_rows[None, :] < WINDOW)
    )


MESH_ID = pl.DeviceIdType.MESH
GELU_A = 0.7978845608028654
GELU_B = 0.044715
TILE = 256


def ring_step(size):
    here = lax.axis_index("z")
    return lax.rem(here + 1, size)


def other_half():
    return 1 - lax.axis_index("mp")


def remote(src, dst, send_sem, recv_sem, where):
    return pltpu.make_async_remote_copy(
        src_ref=src,
        dst_ref=dst,
        send_sem=send_sem,
        recv_sem=recv_sem,
        device_id=where,
        device_id_type=MESH_ID,
    )


def dot_nn(left, right):
    return lax.dot_general(
        left, right, (((1,), (0,)), ((), ())), preferred_element_type=jnp.float32
    )


def gelu_parts(gate):
    square = gate * gate
    bend = jnp.tanh(GELU_A * gate * (1.0 + GELU_B * square))
    half = 0.5 * (1.0 + bend)
    slope = half + 0.5 * gate * (1.0 - bend * bend) * GELU_A * (1.0 + 3.0 * GELU_B * square)
    return gate * half, slope


def ffn_kernel(
    z_size,
    own_ref,
    dy_hbm,
    w_hbm,
    gn_ref,
    mix_ref,
    grads_hbm,
    n2,
    dy,
    w3,
    h3,
    gn_part,
    mix_part,
    gn_y,
    mix_y,
    gn_z,
    mix_z,
    gn_s,
    mix_s,
    load_sem,
    ag_y_send,
    ag_y_recv,
    ag_z_send,
    ag_z_recv,
    rs_y_send,
    rs_y_recv,
    rs_z_send,
    rs_z_recv,
    out_sem,
):
    own = own_ref.shape[0]
    width = own_ref.shape[1]
    units = w3.shape[2]
    me_y = lax.axis_index("mp")
    me_z = lax.axis_index("z")
    mine = pl.ds(pl.multiple_of(me_y * own, own), own)
    theirs = pl.ds(pl.multiple_of((1 - me_y) * own, own), own)
    to_y = {"mp": 1 - me_y}
    to_z = {"z": lax.rem(me_z + 1, z_size)}
    from_z = {"z": lax.rem(me_z + z_size - 1, z_size)}

    loads = []
    for index in range(z_size):
        loads.append(
            pltpu.make_async_copy(
                dy_hbm.at[lax.rem(me_z - index + z_size, z_size)], dy.at[index], load_sem.at[index]
            )
        )
    for index in range(3):
        loads.append(
            pltpu.make_async_copy(w_hbm.at[index], w3.at[index], load_sem.at[z_size + index])
        )
    for load in loads:
        load.start()

    barrier = pltpu.get_barrier_semaphore()
    for where in (to_y, to_z, from_z):
        pl.semaphore_signal(barrier, inc=1, device_id=where, device_id_type=MESH_ID)
    pl.semaphore_wait(barrier, 3)

    def ag_y(index):
        src = own_ref if index == 0 else n2.at[index, mine]
        return remote(src, n2.at[index, mine], ag_y_send.at[index], ag_y_recv.at[index], to_y)

    def ag_y_in(index):
        return remote(
            n2.at[index, theirs], n2.at[index, theirs], ag_y_send.at[index], ag_y_recv.at[index], to_y
        )

    def ag_z(index):
        src = own_ref if index == 0 else n2.at[index, mine]
        return remote(
            src, n2.at[index + 1, mine], ag_z_send.at[index], ag_z_recv.at[index + 1], to_z
        )

    def ag_z_in(index):
        return remote(
            n2.at[index, mine], n2.at[index, mine], ag_z_send.at[0], ag_z_recv.at[index], to_z
        )

    def forward(index):
        ag_z_in(index).wait_recv()
        if index < z_size - 1:
            ag_z(index).start()
        ag_y(index).start()

    ag_y(0).start()
    ag_z(0).start()
    n2[0, mine, :] = own_ref[...]

    def chunk(index):
        ag_y_in(index).wait_recv()
        base = index * 2 * own
        rows = pl.ds(base, 2 * own)

        def up_tile(tile, carry):
            cols = pl.ds(pl.multiple_of(tile * TILE, TILE), TILE)
            normed = n2[index]
            gate = dot_nn(normed, w3[0, :, cols])
            up_proj = dot_nn(normed, w3[1, :, cols])
            grad_hidden = dot_nn(dy[index], w3[2, :, cols])
            act, slope = gelu_parts(gate)
            h3[0, rows, cols] = (grad_hidden * up_proj * slope).astype(jnp.bfloat16)
            h3[1, rows, cols] = (grad_hidden * act).astype(jnp.bfloat16)
            h3[2, rows, cols] = (act * up_proj).astype(jnp.bfloat16)
            return carry

        lax.fori_loop(0, units // TILE, up_tile, 0)

        def down_tile(tile, carry):
            cols = pl.ds(pl.multiple_of(tile * TILE, TILE), TILE)
            gn_part[index, :, cols] = (
                matmul_nt(h3[0, rows, :], w3[0, cols, :]) + matmul_nt(h3[1, rows, :], w3[1, cols, :])
            ).astype(jnp.bfloat16)
            mix_part[index, :, cols] = matmul_nt(h3[2, rows, :], w3[2, cols, :]).astype(
                jnp.bfloat16
            )
            return carry

        lax.fori_loop(0, width // TILE, down_tile, 0)

    sums = ((gn_part, gn_y, gn_z, gn_s), (mix_part, mix_y, mix_z, mix_s))

    def rs_y(kind, index):
        part, from_y, _, _ = sums[kind]
        return remote(
            part.at[index, theirs],
            from_y.at[index],
            rs_y_send.at[kind, index],
            rs_y_recv.at[kind, index],
            to_y,
        )

    def rs_z(kind, index):
        _, _, arrived, leaving = sums[kind]
        slot = (index + 1) % z_size
        return remote(
            leaving.at[index],
            arrived.at[slot],
            rs_z_send.at[kind, index],
            rs_z_recv.at[kind, slot],
            to_z,
        )

    def rs_z_in(kind, index):
        _, _, arrived, leaving = sums[kind]
        return remote(
            leaving.at[1],
            arrived.at[index],
            rs_z_send.at[kind, 1],
            rs_z_recv.at[kind, index],
            to_z,
        )

    def rs_step(kind, index, out_ref):
        part, from_y, arrived, leaving = sums[kind]
        rs_y(kind, index).wait_recv()
        if index != 1:
            rs_z_in(kind, index).wait_recv()

        def add_tile(tile, carry):
            cols = pl.ds(pl.multiple_of(tile * TILE, TILE), TILE)
            total = part[index, mine, cols].astype(jnp.float32) + from_y[index, :, cols].astype(
                jnp.float32
            )
            if index != 1:
                total = total + arrived[index, :, cols].astype(jnp.float32)
            if index == 0:
                out_ref[:, cols] = total
            else:
                leaving[index, :, cols] = total.astype(jnp.bfloat16)
            return carry

        lax.fori_loop(0, width // TILE, add_tile, 0)
        if index != 0:
            rs_z(kind, index).start()

    out_copies = []

    def grad_tiles(first, last):
        def tile_body(tile, carry):
            cols = pl.ds(pl.multiple_of(tile * TILE, TILE), TILE)
            left = n2[:, :, cols].reshape(z_size * 2 * own, TILE).T
            for kind in range(2):
                w3[kind, cols, :] = dot_nn(left, h3[kind]).astype(jnp.bfloat16)
            left = dy[:, :, cols].reshape(z_size * 2 * own, TILE).T
            w3[2, cols, :] = dot_nn(left, h3[2]).astype(jnp.bfloat16)
            return carry

        lax.fori_loop(first, last, tile_body, 0)
        span = pl.ds(first * TILE, (last - first) * TILE)
        for kind in range(3):
            copy = pltpu.make_async_copy(
                w3.at[kind, span], grads_hbm.at[kind, span], out_sem.at[len(out_copies)]
            )
            copy.start()
            out_copies.append(copy)

    forward(1)
    for load in loads:
        load.wait()
    chunk(0)
    rs_y(0, 0).start()
    forward(2)
    chunk(1)
    rs_y(0, 1).start()
    forward(3)
    chunk(2)
    rs_y(0, 2).start()
    rs_step(0, 1, gn_ref)
    chunk(3)
    rs_y(0, 3).start()
    for index in (1, 2, 3, 0):
        rs_y(1, index).start()
    rs_step(0, 2, gn_ref)
    tiles = width // TILE
    marks = [0, tiles // 4, tiles // 2, (3 * tiles) // 4, tiles]
    grad_tiles(marks[0], marks[1])
    rs_step(0, 3, gn_ref)
    grad_tiles(marks[1], marks[2])
    rs_step(1, 1, mix_ref)
    grad_tiles(marks[2], marks[3])
    rs_step(0, 0, gn_ref)
    rs_step(1, 2, mix_ref)
    grad_tiles(marks[3], marks[4])
    rs_step(1, 3, mix_ref)
    rs_step(1, 0, mix_ref)

    for index in range(z_size):
        ag_y(index).wait_send()
        if index < z_size - 1:
            ag_z(index).wait_send()
        for kind in range(2):
            rs_y(kind, index).wait_send()
            if index != 0:
                rs_z(kind, index).wait_send()
    for copy in out_copies:
        copy.wait()


def ffn_call(normed, grad_all, weights):
    z_size = lax.axis_size("z")
    own, width = normed.shape
    units = weights.shape[2]
    pair = 2 * own
    wide = lambda *lead: pltpu.VMEM((*lead, width), jnp.bfloat16)
    dma = lambda *lead: pltpu.SemaphoreType.DMA(lead)
    vmem = pl.BlockSpec(memory_space=pltpu.VMEM)
    hbm = pl.BlockSpec(memory_space=pl.ANY)
    return pl.pallas_call(
        functools.partial(ffn_kernel, z_size),
        out_shape=(
            jax.ShapeDtypeStruct((own, width), jnp.float32),
            jax.ShapeDtypeStruct((own, width), jnp.float32),
            jax.ShapeDtypeStruct(weights.shape, jnp.bfloat16),
        ),
        in_specs=[vmem, hbm, hbm],
        out_specs=(vmem, vmem, hbm),
        scratch_shapes=[
            wide(z_size, pair),
            wide(z_size, pair),
            pltpu.VMEM(weights.shape, jnp.bfloat16),
            pltpu.VMEM((3, z_size * pair, units), jnp.bfloat16),
            wide(z_size, pair),
            wide(z_size, pair),
            wide(z_size, own),
            wide(z_size, own),
            wide(z_size, own),
            wide(z_size, own),
            wide(z_size, own),
            wide(z_size, own),
            dma(z_size + 3),
            dma(z_size),
            dma(z_size),
            dma(z_size),
            dma(z_size),
            dma(2, z_size),
            dma(2, z_size),
            dma(2, z_size),
            dma(2, z_size),
            dma(12),
        ],
        compiler_params=pltpu.CompilerParams(
            collective_id=0, has_side_effects=True, vmem_limit_bytes=VMEM_BYTES
        ),
        cost_estimate=pl.CostEstimate(
            flops=18 * z_size * pair * width * units,
            bytes_accessed=4 * weights.size + 12 * z_size * pair * width,
            transcendentals=z_size * pair * units,
        ),
    )(normed, grad_all, weights)


FF_SPLIT = 4


def shards(
    tokens,
    segments,
    positions,
    cotangent,
    attn_gain,
    ffn_gain,
    w_kv,
    w_query,
    w_out,
    w_gate,
    w_up,
    w_down,
):
    everywhere = ("z", "xc", "mp")
    dp = ("z", "xc")
    z_size = lax.axis_size("z")
    xc_size = lax.axis_size("xc")
    gains = lax.all_gather(
        jnp.stack([attn_gain, ffn_gain], axis=1), everywhere, axis=0, tiled=True
    ).astype(jnp.float32)
    gain_one, gain_two = gains[:, 0], gains[:, 1]
    kv_weight = lax.all_gather(w_kv, everywhere, axis=0, tiled=True)
    head_dim = kv_weight.shape[1] // 2
    width = tokens.shape[1]
    seq_len = segments.shape[0]
    heads_here = w_query.shape[1] // head_dim
    scale = head_dim ** (-0.5)
    cosine, sine = rotary_angles(positions, head_dim)
    inputs_f = tokens.astype(jnp.float32)
    tokens_all = lax.all_gather(tokens, "mp", axis=0, tiled=True)
    normed_one = norm_gain(tokens_all.astype(jnp.float32), gain_one).astype(jnp.bfloat16)
    query_weight = lax.all_gather(w_query, dp, axis=0, tiled=True)
    out_weight = lax.all_gather(w_out, dp, axis=0, tiled=True)

    rows = w_gate.shape[0]
    unit = w_gate.shape[1] // z_size
    units = -(-unit // TILE) * TILE

    def spread(weight):
        pieces = weight.reshape(rows, z_size, unit).transpose(1, 0, 2)
        pieces = jnp.pad(pieces, ((0, 0), (0, 0), (0, units - unit)))
        pieces = lax.all_to_all(pieces, "z", split_axis=0, concat_axis=0, tiled=True)
        return lax.all_gather(pieces, "xc", axis=1, tiled=False).reshape(width, units)

    ffn_weights = jnp.stack([spread(w_gate), spread(w_up), spread(w_down)])
    grad_all = lax.all_gather(cotangent, ("z", "mp"), axis=0, tiled=True)
    grad_all = grad_all.reshape(z_size, seq_len, width)

    query = jnp.dot(normed_one, query_weight, preferred_element_type=jnp.float32).reshape(
        seq_len, heads_here, head_dim
    )
    rotated = (rotate(query, cosine[:, None], sine[:, None]) * scale).astype(jnp.bfloat16)
    keyval = jnp.dot(normed_one, kv_weight, preferred_element_type=jnp.float32)
    keys = rotate(keyval[:, :head_dim], cosine, sine).astype(jnp.bfloat16)
    values = keyval[:, head_dim:].astype(jnp.bfloat16)
    allowed = block_allowed(segments, 0, seq_len)
    scores = jnp.einsum("thd,sd->hts", rotated, keys, preferred_element_type=jnp.float32)
    scores = jnp.where(allowed[None], scores, masked_score)
    row_max = jnp.max(scores, axis=-1, keepdims=True)
    weights = jnp.exp(scores - row_max)
    probs = weights / jnp.sum(weights, axis=-1, keepdims=True)
    probs_low = probs.astype(jnp.bfloat16)
    attn_vals = (
        jnp.einsum("hts,sd->thd", probs_low, values, preferred_element_type=jnp.float32)
        .reshape(seq_len, heads_here * head_dim)
        .astype(jnp.bfloat16)
    )
    mid = inputs_f + lax.psum_scatter(
        matmul_nt(attn_vals, out_weight).astype(jnp.bfloat16),
        "mp",
        scatter_dimension=0,
        tiled=True,
    ).astype(jnp.float32)
    normed_two = norm_gain(mid, gain_two).astype(jnp.bfloat16)
    grad_normed_two, mixed_sum, weight_parts = ffn_call(normed_two, grad_all, ffn_weights)
    mixed = (mid + mixed_sum).astype(jnp.bfloat16)

    def collect(part):
        pieces = part.reshape(z_size, xc_size, rows, units).transpose(1, 0, 2, 3)
        pieces = pieces.reshape(xc_size * z_size * rows, units)
        pieces = lax.psum_scatter(pieces, "xc", scatter_dimension=0, tiled=True)
        pieces = pieces.reshape(z_size, rows, units)
        pieces = lax.all_to_all(pieces, "z", split_axis=0, concat_axis=0, tiled=True)
        pieces = pieces[:, :, :unit]
        return pieces.transpose(1, 0, 2).reshape(rows, z_size * unit).astype(jnp.float32)

    w_gate_grad, w_up_grad, w_down_grad = [collect(weight_parts[kind]) for kind in range(3)]

    norm_pull_two = jax.vjp(norm_gain, mid, gain_two)[1]
    grad_mid_norm, grad_gain_two = norm_pull_two(grad_normed_two)
    grad_mid = cotangent.astype(jnp.float32) + grad_mid_norm
    grad_mid_all = lax.all_gather(grad_mid.astype(jnp.bfloat16), "mp", axis=0, tiled=True)
    grad_vals = (
        jnp.dot(grad_mid_all, out_weight, preferred_element_type=jnp.float32)
        .astype(jnp.bfloat16)
        .reshape(seq_len, heads_here, head_dim)
    )
    grad_probs = jnp.einsum("thd,sd->hts", grad_vals, values, preferred_element_type=jnp.float32)
    delta = jnp.sum(probs * grad_probs, axis=-1, keepdims=True)
    grad_scores = (probs * (grad_probs - delta)).astype(jnp.bfloat16)
    grad_rot = jnp.einsum("hts,sd->thd", grad_scores, keys, preferred_element_type=jnp.float32)
    key_sum = jnp.einsum("hts,thd->sd", grad_scores, rotated, preferred_element_type=jnp.float32)
    value_sum = jnp.einsum("hts,thd->sd", probs_low, grad_vals, preferred_element_type=jnp.float32)
    grad_query = (
        (unrotate(grad_rot, cosine[:, None], sine[:, None]) * scale)
        .reshape(seq_len, heads_here * head_dim)
        .astype(jnp.bfloat16)
    )
    grad_kv = jnp.concatenate([unrotate(key_sum, cosine, sine), value_sum], axis=1).astype(
        jnp.bfloat16
    )
    grad_normed_one = lax.psum_scatter(
        (matmul_nt(grad_query, query_weight) + matmul_nt(grad_kv, kv_weight)).astype(jnp.bfloat16),
        "mp",
        scatter_dimension=0,
        tiled=True,
    ).astype(jnp.float32)
    norm_pull_one = jax.vjp(norm_gain, inputs_f, gain_one)[1]
    grad_input_norm, grad_gain_one = norm_pull_one(grad_normed_one)
    tokens_grad = (grad_mid + grad_input_norm).astype(jnp.bfloat16)

    w_query_grad = lax.psum_scatter(
        matmul_tn(normed_one, grad_query).astype(jnp.bfloat16), dp, scatter_dimension=0, tiled=True
    ).astype(jnp.float32)
    w_out_grad = lax.psum_scatter(
        matmul_tn(grad_mid_all, attn_vals).astype(jnp.bfloat16), dp, scatter_dimension=0, tiled=True
    ).astype(jnp.float32)
    small = jnp.concatenate(
        [matmul_tn(normed_one, grad_kv), grad_gain_one[:, None], grad_gain_two[:, None]], axis=1
    )
    small = lax.psum_scatter(small, everywhere, scatter_dimension=0, tiled=True)
    kv_grad = small[:, : 2 * head_dim]
    return (
        mixed,
        tokens_grad,
        small[:, 2 * head_dim],
        small[:, 2 * head_dim + 1],
        kv_grad,
        w_query_grad,
        w_out_grad,
        w_gate_grad,
        w_up_grad,
        w_down_grad,
    )


def solution(mesh):
    dp_size, mp_size = mesh.shape["dp"], mesh.shape["mp"]
    fine = jax.sharding.Mesh(
        mesh.devices.reshape(FF_SPLIT, dp_size // FF_SPLIT, mp_size), ("z", "xc", "mp")
    )
    dp = ("z", "xc")
    all_axes = ("z", "xc", "mp")
    in_specs = (
        P(all_axes, None),
        P(dp),
        P(dp),
        P(all_axes, None),
        P(all_axes),
        P(all_axes),
        P(all_axes, None),
        P(dp, "mp"),
        P(dp, "mp"),
        P(dp, "mp"),
        P(dp, "mp"),
        P(dp, "mp"),
    )
    out_specs = (
        P(all_axes, None),
        P(all_axes, None),
        P(all_axes),
        P(all_axes),
        P(all_axes, None),
        P(dp, "mp"),
        P(dp, "mp"),
        P(dp, "mp"),
        P(dp, "mp"),
        P(dp, "mp"),
    )
    return jax.shard_map(shards, mesh=fine, in_specs=in_specs, out_specs=out_specs, check_vma=False)
```

```python
import functools

import jax
import jax.numpy as jnp
from jax import lax
from jax.experimental import pallas as pl
from jax.experimental.pallas import tpu as pltpu
from jax.sharding import PartitionSpec as P

WINDOW = 2048


epsilon = 1e-06
rope_base = 10000.0
masked_score = -1e30
VMEM_BYTES = 62 * 1024 * 1024


def norm_gain(values, gain):
    return values * lax.rsqrt(jnp.mean(values * values, axis=-1, keepdims=True) + epsilon) * gain


def rotary_angles(positions, head_width):
    quarter = head_width // 4
    freqs = rope_base ** (-jnp.arange(quarter).astype(jnp.float32) / quarter)
    phase = positions.astype(jnp.float32)[:, None] * freqs[None, :]
    return (jnp.cos(phase), jnp.sin(phase))


def rotate(values, cosine, sine):
    quarter = cosine.shape[-1]
    first_half = values[..., :quarter]
    second_half = values[..., quarter : 2 * quarter]
    return jnp.concatenate(
        [
            first_half * cosine - second_half * sine,
            second_half * cosine + first_half * sine,
            values[..., 2 * quarter :],
        ],
        axis=-1,
    )


def unrotate(values, cosine, sine):
    quarter = cosine.shape[-1]
    first_half = values[..., :quarter]
    second_half = values[..., quarter : 2 * quarter]
    return jnp.concatenate(
        [
            first_half * cosine + second_half * sine,
            second_half * cosine - first_half * sine,
            values[..., 2 * quarter :],
        ],
        axis=-1,
    )


def gelu_product(gate, up_proj):
    return jax.nn.gelu(gate, approximate=True) * up_proj


def matmul_nt(left, right):
    return lax.dot_general(
        left, right, (((1,), (1,)), ((), ())), preferred_element_type=jnp.float32
    )


def matmul_tn(left, right):
    return lax.dot_general(
        left, right, (((0,), (0,)), ((), ())), preferred_element_type=jnp.float32
    )


def block_allowed(segments, first_row, rows):
    seq_len = segments.shape[0]
    query_rows = first_row + jnp.arange(rows)
    key_rows = jnp.arange(seq_len)
    return (
        (segments[:, None] == segments[None, :])
        & (key_rows[None, :] <= query_rows[:, None])
        & (query_rows[:, None] - key_rows[None, :] < WINDOW)
    )


MESH_ID = pl.DeviceIdType.MESH
GELU_A = 0.7978845608028654
GELU_B = 0.044715
TILE = 256


def ring_step(size):
    here = lax.axis_index("z")
    return lax.rem(here + 1, size)


def other_half():
    return 1 - lax.axis_index("mp")


def remote(src, dst, send_sem, recv_sem, where):
    return pltpu.make_async_remote_copy(
        src_ref=src,
        dst_ref=dst,
        send_sem=send_sem,
        recv_sem=recv_sem,
        device_id=where,
        device_id_type=MESH_ID,
    )


def dot_nn(left, right):
    return lax.dot_general(
        left, right, (((1,), (0,)), ((), ())), preferred_element_type=jnp.float32
    )


def gelu_parts(gate):
    square = gate * gate
    bend = jnp.tanh(GELU_A * gate * (1.0 + GELU_B * square))
    half = 0.5 * (1.0 + bend)
    slope = half + 0.5 * gate * (1.0 - bend * bend) * GELU_A * (1.0 + 3.0 * GELU_B * square)
    return gate * half, slope


def ffn_kernel(
    z_size,
    main,
    own_ref,
    dy_hbm,
    w_hbm,
    gn_ref,
    mix_ref,
    grads_hbm,
    n2,
    dy,
    w3,
    h3,
    gn_part,
    mix_part,
    gn_y,
    mix_y,
    gn_z,
    mix_z,
    gn_s,
    mix_s,
    load_sem,
    ag_y_send,
    ag_y_recv,
    ag_z_send,
    ag_z_recv,
    rs_y_send,
    rs_y_recv,
    rs_z_send,
    rs_z_recv,
    out_sem,
):
    own = own_ref.shape[0]
    width = own_ref.shape[1]
    units = w3.shape[2]
    me_y = lax.axis_index("mp")
    me_z = lax.axis_index("z")
    mine = pl.ds(pl.multiple_of(me_y * own, own), own)
    theirs = pl.ds(pl.multiple_of((1 - me_y) * own, own), own)
    to_y = {"mp": 1 - me_y}
    to_z = {"z": lax.rem(me_z + 1, z_size)}
    from_z = {"z": lax.rem(me_z + z_size - 1, z_size)}

    loads = []
    for index in range(z_size):
        place = index if main else lax.rem(me_z - index + z_size, z_size)
        loads.append(pltpu.make_async_copy(dy_hbm.at[place], dy.at[index], load_sem.at[index]))
    for index in range(3):
        loads.append(
            pltpu.make_async_copy(w_hbm.at[index], w3.at[index], load_sem.at[z_size + index])
        )
    for load in loads:
        load.start()

    barrier = pltpu.get_barrier_semaphore()
    for where in (to_y, to_z, from_z):
        pl.semaphore_signal(barrier, inc=1, device_id=where, device_id_type=MESH_ID)
    pl.semaphore_wait(barrier, 3)

    def ag_y(index):
        src = own_ref if index == 0 else n2.at[index, mine]
        return remote(src, n2.at[index, mine], ag_y_send.at[index], ag_y_recv.at[index], to_y)

    def ag_y_in(index):
        return remote(
            n2.at[index, theirs], n2.at[index, theirs], ag_y_send.at[index], ag_y_recv.at[index], to_y
        )

    def ag_z(index):
        src = own_ref if index == 0 else n2.at[index, mine]
        return remote(
            src, n2.at[index + 1, mine], ag_z_send.at[index], ag_z_recv.at[index + 1], to_z
        )

    def ag_z_in(index):
        return remote(
            n2.at[index, mine], n2.at[index, mine], ag_z_send.at[0], ag_z_recv.at[index], to_z
        )

    def forward(index):
        ag_z_in(index).wait_recv()
        if index < z_size - 1:
            ag_z(index).start()
        ag_y(index).start()

    ag_y(0).start()
    ag_z(0).start()
    n2[0, mine, :] = own_ref[...]

    def chunk(index):
        ag_y_in(index).wait_recv()
        base = index * 2 * own
        rows = pl.ds(base, 2 * own)

        def up_tile(tile, carry):
            cols = pl.ds(pl.multiple_of(tile * TILE, TILE), TILE)
            normed = n2[index]
            gate = dot_nn(normed, w3[0, :, cols])
            up_proj = dot_nn(normed, w3[1, :, cols])
            grad_hidden = dot_nn(dy[index], w3[2, :, cols])
            act, slope = gelu_parts(gate)
            if main:
                at = lax.broadcasted_iota(jnp.int32, (1, TILE), 1) + tile * TILE
                low_at = main + 64 * lax.rem(me_z, 2)
                keep = (at < main) | ((at >= low_at) & (at < low_at + 64))
                act = jnp.where(keep, act, 0.0)
                slope = jnp.where(keep, slope, 0.0)
            h3[0, rows, cols] = (grad_hidden * up_proj * slope).astype(jnp.bfloat16)
            h3[1, rows, cols] = (grad_hidden * act).astype(jnp.bfloat16)
            h3[2, rows, cols] = (act * up_proj).astype(jnp.bfloat16)
            return carry

        lax.fori_loop(0, units // TILE, up_tile, 0)

        def down_tile(tile, carry):
            cols = pl.ds(pl.multiple_of(tile * TILE, TILE), TILE)
            gn_part[index, :, cols] = (
                matmul_nt(h3[0, rows, :], w3[0, cols, :]) + matmul_nt(h3[1, rows, :], w3[1, cols, :])
            ).astype(jnp.bfloat16)
            mix_part[index, :, cols] = matmul_nt(h3[2, rows, :], w3[2, cols, :]).astype(
                jnp.bfloat16
            )
            return carry

        lax.fori_loop(0, width // TILE, down_tile, 0)

    sums = ((gn_part, gn_y, gn_z, gn_s), (mix_part, mix_y, mix_z, mix_s))

    def rs_y(kind, index):
        part, from_y, _, _ = sums[kind]
        return remote(
            part.at[index, theirs],
            from_y.at[index],
            rs_y_send.at[kind, index],
            rs_y_recv.at[kind, index],
            to_y,
        )

    def rs_z(kind, index):
        _, _, arrived, leaving = sums[kind]
        slot = (index + 1) % z_size
        return remote(
            leaving.at[index],
            arrived.at[slot],
            rs_z_send.at[kind, index],
            rs_z_recv.at[kind, slot],
            to_z,
        )

    def rs_z_in(kind, index):
        _, _, arrived, leaving = sums[kind]
        return remote(
            leaving.at[1],
            arrived.at[index],
            rs_z_send.at[kind, 1],
            rs_z_recv.at[kind, index],
            to_z,
        )

    def rs_step(kind, index, out_ref):
        part, from_y, arrived, leaving = sums[kind]
        rs_y(kind, index).wait_recv()
        if index != 1:
            rs_z_in(kind, index).wait_recv()

        def add_tile(tile, carry):
            cols = pl.ds(pl.multiple_of(tile * TILE, TILE), TILE)
            total = part[index, mine, cols].astype(jnp.float32) + from_y[index, :, cols].astype(
                jnp.float32
            )
            if index != 1:
                total = total + arrived[index, :, cols].astype(jnp.float32)
            if index == 0:
                out_ref[:, cols] = total
            else:
                leaving[index, :, cols] = total.astype(jnp.bfloat16)
            return carry

        lax.fori_loop(0, width // TILE, add_tile, 0)
        if index != 0:
            rs_z(kind, index).start()

    out_copies = []

    def grad_tiles(first, last):
        def tile_body(tile, carry):
            cols = pl.ds(pl.multiple_of(tile * TILE, TILE), TILE)
            left = n2[:, :, cols].reshape(z_size * 2 * own, TILE).T
            for kind in range(2):
                w3[kind, cols, :] = dot_nn(left, h3[kind]).astype(jnp.bfloat16)
            left = dy[:, :, cols].reshape(z_size * 2 * own, TILE).T
            w3[2, cols, :] = dot_nn(left, h3[2]).astype(jnp.bfloat16)
            return carry

        lax.fori_loop(first, last, tile_body, 0)
        span = pl.ds(first * TILE, (last - first) * TILE)
        for kind in range(3):
            copy = pltpu.make_async_copy(
                w3.at[kind, span], grads_hbm.at[kind, span], out_sem.at[len(out_copies)]
            )
            copy.start()
            out_copies.append(copy)

    forward(1)
    for load in loads:
        load.wait()
    chunk(0)
    rs_y(0, 0).start()
    forward(2)
    chunk(1)
    rs_y(0, 1).start()
    forward(3)
    chunk(2)
    rs_y(0, 2).start()
    rs_step(0, 1, gn_ref)
    chunk(3)
    rs_y(0, 3).start()
    for index in (1, 2, 3, 0):
        rs_y(1, index).start()
    rs_step(0, 2, gn_ref)
    tiles = width // TILE
    marks = [0, tiles // 4, tiles // 2, (3 * tiles) // 4, tiles]
    grad_tiles(marks[0], marks[1])
    rs_step(0, 3, gn_ref)
    grad_tiles(marks[1], marks[2])
    rs_step(1, 1, mix_ref)
    grad_tiles(marks[2], marks[3])
    rs_step(0, 0, gn_ref)
    rs_step(1, 2, mix_ref)
    grad_tiles(marks[3], marks[4])
    rs_step(1, 3, mix_ref)
    rs_step(1, 0, mix_ref)

    for index in range(z_size):
        ag_y(index).wait_send()
        if index < z_size - 1:
            ag_z(index).wait_send()
        for kind in range(2):
            rs_y(kind, index).wait_send()
            if index != 0:
                rs_z(kind, index).wait_send()
    for copy in out_copies:
        copy.wait()


def ffn_call(normed, grad_all, weights, main):
    z_size = lax.axis_size("z")
    own, width = normed.shape
    units = weights.shape[2]
    pair = 2 * own
    wide = lambda *lead: pltpu.VMEM((*lead, width), jnp.bfloat16)
    dma = lambda *lead: pltpu.SemaphoreType.DMA(lead)
    vmem = pl.BlockSpec(memory_space=pltpu.VMEM)
    hbm = pl.BlockSpec(memory_space=pl.ANY)
    return pl.pallas_call(
        functools.partial(ffn_kernel, z_size, main),
        out_shape=(
            jax.ShapeDtypeStruct((own, width), jnp.float32),
            jax.ShapeDtypeStruct((own, width), jnp.float32),
            jax.ShapeDtypeStruct(weights.shape, jnp.bfloat16),
        ),
        in_specs=[vmem, hbm, hbm],
        out_specs=(vmem, vmem, hbm),
        scratch_shapes=[
            wide(z_size, pair),
            wide(z_size, pair),
            pltpu.VMEM(weights.shape, jnp.bfloat16),
            pltpu.VMEM((3, z_size * pair, units), jnp.bfloat16),
            wide(z_size, pair),
            wide(z_size, pair),
            wide(z_size, own),
            wide(z_size, own),
            wide(z_size, own),
            wide(z_size, own),
            wide(z_size, own),
            wide(z_size, own),
            dma(z_size + 3),
            dma(z_size),
            dma(z_size),
            dma(z_size),
            dma(z_size),
            dma(2, z_size),
            dma(2, z_size),
            dma(2, z_size),
            dma(2, z_size),
            dma(12),
        ],
        compiler_params=pltpu.CompilerParams(
            collective_id=0, has_side_effects=True, vmem_limit_bytes=VMEM_BYTES
        ),
        cost_estimate=pl.CostEstimate(
            flops=18 * z_size * pair * width * units,
            bytes_accessed=4 * weights.size + 12 * z_size * pair * width,
            transcendentals=z_size * pair * units,
        ),
    )(normed, grad_all, weights)


def spin(values, table):
    first = values[:, : values.shape[1] // 2]
    turned = first * table[0] + pltpu.roll(first, first.shape[1] // 2, 1) * table[1]
    return jnp.concatenate([turned, values[:, values.shape[1] // 2 :]], axis=1)


def spin_back(values, table):
    first = values[:, : values.shape[1] // 2]
    turned = first * table[0] - pltpu.roll(first, first.shape[1] // 2, 1) * table[1]
    return jnp.concatenate([turned, values[:, values.shape[1] // 2 :]], axis=1)


def head_probs(rotated, keys, allowed):
    scores = jnp.where(allowed > 0.5, matmul_nt(rotated, keys), masked_score)
    weights = jnp.exp(scores - jnp.max(scores, axis=-1, keepdims=True))
    return weights / jnp.sum(weights, axis=-1, keepdims=True)


def ragged_split(columns, parts):
    main = columns // parts // 128 * 128
    return main, main + 128


def pre_kernel(
    z_size,
    tok_ref,
    kvg_ref,
    table_ref,
    allow_ref,
    cot_hbm,
    wq_hbm,
    wo_hbm,
    wg_hbm,
    wu_hbm,
    wd_hbm,
    n1_ref,
    rot_ref,
    key_ref,
    val_ref,
    att_ref,
    mid_ref,
    n2_ref,
    gain_ref,
    kv_out,
    wq_out,
    wo_out,
    w3_out,
    dy_out,
    kv_w,
    q_w,
    o_w,
    tok,
    part,
    part_y,
    y_send,
    y_recv,
    az_send,
    az_recv,
    ax_send,
    ax_recv,
    ac_send,
    ac_recv,
    fz_send,
    fz_recv,
    fx_send,
    fx_recv,
    fc_send,
    fc_recv,
    dz_send,
    dz_recv,
    dy_send,
    dy_recv,
    local_sem,
):
    me_z, me_x = lax.axis_index("z"), lax.axis_index("x")
    me_c, me_y = lax.axis_index("c"), lax.axis_index("mp")
    own, width = tok_ref.shape
    rows = wq_hbm.shape[0]
    half_rows = kvg_ref.shape[0]
    head = key_ref.shape[1]
    main, units = ragged_split(wg_hbm.shape[1], z_size)
    to_y, to_x, to_c = {"mp": 1 - me_y}, {"x": 1 - me_x}, {"c": 1 - me_c}

    def to_z(step):
        return {"z": lax.rem(me_z + step, z_size)}

    def from_z(step):
        return lax.rem(me_z - step + z_size, z_size)

    def row_block(step, x_at, c_at):
        start = ((from_z(step) * 2 + x_at) * 2 + c_at) * rows
        return pl.ds(pl.multiple_of(start, rows), rows)

    mine = pl.ds(pl.multiple_of(me_y * own, own), own)
    theirs = pl.ds(pl.multiple_of((1 - me_y) * own, own), own)
    bufs = (kv_w, q_w, o_w)
    inputs = (None, wq_hbm, wo_hbm)

    locals_ = []

    def local(src, dst):
        copy = pltpu.make_async_copy(src, dst, local_sem.at[len(locals_)])
        copy.start()
        locals_.append(copy)
        return copy

    here = row_block(0, me_x, me_c)
    own_q = local(wq_hbm, q_w.at[here])
    own_o = local(wo_hbm, o_w.at[here])
    ffn_in = (wg_hbm, wu_hbm, wd_hbm)

    def pieces(target):
        yield pl.ds(pl.multiple_of(target * main, 128), main), pl.ds(0, main)
        tail = (z_size * main) + (target // 2) * 128
        yield pl.ds(pl.multiple_of(tail, 128), 128), pl.ds(main, 128)

    own_f = []
    for kind in range(3):
        for src, dst in pieces(me_z):
            own_f.append(local(ffn_in[kind].at[:, src], w3_out.at[kind, here, dst]))
    own_d = local(cot_hbm, dy_out.at[0, mine])

    barrier = pltpu.get_barrier_semaphore()
    peers = [to_y, to_x, to_c] + [to_z(step) for step in range(1, z_size)]
    for where in peers:
        pl.semaphore_signal(barrier, inc=1, device_id=where, device_id_type=MESH_ID)
    pl.semaphore_wait(barrier, len(peers))

    kv_mine = pl.ds(pl.multiple_of(here.start + me_y * half_rows, half_rows), half_rows)
    kv_theirs = pl.ds(pl.multiple_of(here.start + (1 - me_y) * half_rows, half_rows), half_rows)
    kv_y = remote(kvg_ref, kv_w.at[kv_mine], y_send.at[0], y_recv.at[0], to_y)
    kv_y_in = remote(kvg_ref, kv_w.at[kv_theirs], y_send.at[0], y_recv.at[0], to_y)
    tok_y = remote(tok_ref, tok.at[mine], y_send.at[1], y_recv.at[1], to_y)
    tok_y_in = remote(tok_ref, tok.at[theirs], y_send.at[1], y_recv.at[1], to_y)
    part_out = remote(part.at[theirs], part_y, y_send.at[2], y_recv.at[2], to_y)

    def source(kind, step):
        if step == 0 and kind:
            return inputs[kind]
        return bufs[kind].at[row_block(step, me_x, me_c)]

    def a_z(kind, step):
        return remote(
            source(kind, step),
            bufs[kind].at[row_block(step, me_x, me_c)],
            az_send.at[kind, step],
            az_recv.at[kind, step + 1],
            to_z(1),
        )

    def a_z_in(kind, step):
        block = bufs[kind].at[row_block(step, me_x, me_c)]
        return remote(block, block, az_send.at[kind, 0], az_recv.at[kind, step], to_z(1))

    def a_x(kind, step):
        return remote(
            source(kind, step),
            bufs[kind].at[row_block(step, me_x, me_c)],
            ax_send.at[kind, step],
            ax_recv.at[kind, step],
            to_x,
        )

    def a_x_in(kind, step):
        block = bufs[kind].at[row_block(step, 1 - me_x, me_c)]
        return remote(block, block, ax_send.at[kind, step], ax_recv.at[kind, step], to_x)

    def a_c(kind, step, far):
        x_at = 1 - me_x if far else me_x
        block = bufs[kind].at[row_block(step, x_at, me_c)]
        src = block if far else source(kind, step)
        slot = step + z_size * far
        return remote(src, block, ac_send.at[kind, slot], ac_recv.at[kind, slot], to_c)

    def a_c_in(kind, step, far):
        x_at = 1 - me_x if far else me_x
        block = bufs[kind].at[row_block(step, x_at, 1 - me_c)]
        slot = step + z_size * far
        return remote(block, block, ac_send.at[kind, slot], ac_recv.at[kind, slot], to_c)

    def f_z(kind, step):
        target = lax.rem(me_z + step, z_size)
        return [
            remote(
                ffn_in[kind].at[:, src],
                w3_out.at[kind, here, dst],
                fz_send.at[kind, step, index],
                fz_recv.at[kind, step, index],
                to_z(step),
            )
            for index, (src, dst) in enumerate(pieces(target))
        ]

    def f_z_in(kind, step):
        block = row_block(step, me_x, me_c)
        return [
            remote(
                w3_out.at[kind, block, dst],
                w3_out.at[kind, block, dst],
                fz_send.at[kind, step, index],
                fz_recv.at[kind, step, index],
                to_z(step),
            )
            for index, (_, dst) in enumerate(pieces(me_z))
        ]

    def f_x(kind, step):
        block = w3_out.at[kind, row_block(step, me_x, me_c)]
        return remote(block, block, fx_send.at[kind, step], fx_recv.at[kind, step], to_x)

    def f_x_in(kind, step):
        block = w3_out.at[kind, row_block(step, 1 - me_x, me_c)]
        return remote(block, block, fx_send.at[kind, step], fx_recv.at[kind, step], to_x)

    def f_c(kind, step, far):
        block = w3_out.at[kind, row_block(step, 1 - me_x if far else me_x, me_c)]
        slot = step + z_size * far
        return remote(block, block, fc_send.at[kind, slot], fc_recv.at[kind, slot], to_c)

    def f_c_in(kind, step, far):
        block = w3_out.at[kind, row_block(step, 1 - me_x if far else me_x, 1 - me_c)]
        slot = step + z_size * far
        return remote(block, block, fc_send.at[kind, slot], fc_recv.at[kind, slot], to_c)

    def d_source(step):
        return cot_hbm if step == 0 else dy_out.at[step, mine]

    def d_z(step):
        return remote(
            d_source(step), dy_out.at[step + 1, mine], dz_send.at[step], dz_recv.at[step + 1], to_z(1)
        )

    def d_z_in(step):
        block = dy_out.at[step, mine]
        return remote(block, block, dz_send.at[0], dz_recv.at[step], to_z(1))

    def d_y(step):
        return remote(
            d_source(step), dy_out.at[step, mine], dy_send.at[step], dy_recv.at[step], to_y
        )

    def d_y_in(step):
        block = dy_out.at[step, theirs]
        return remote(block, block, dy_send.at[step], dy_recv.at[step], to_y)

    kv_y.start()
    tok_y.start()
    for kind in (1, 2):
        a_z(kind, 0).start()
        a_x(kind, 0).start()
        a_c(kind, 0, 0).start()
    kv_w[kv_mine, :] = kvg_ref[...]
    tok[mine, :] = tok_ref[...]
    kv_y_in.wait_recv()
    a_z(0, 0).start()
    a_x(0, 0).start()
    a_c(0, 0, 0).start()
    d_y(0).start()
    for step in range(1, z_size):
        for kind in (1, 0, 2):
            a_z_in(kind, step).wait_recv()
            if step < z_size - 1:
                a_z(kind, step).start()
            a_x(kind, step).start()
            a_c(kind, step, 0).start()
        if step == z_size - 2:
            for copy in own_f:
                copy.wait()
            for kind in range(3):
                for away in (1, 3, 2):
                    for copy in f_z(kind, away):
                        copy.start()
            d_z(0).start()
        for kind in (1, 0, 2):
            a_x_in(kind, step - 1).wait_recv()
            a_c(kind, step - 1, 1).start()
    for kind in (1, 0, 2):
        a_x_in(kind, z_size - 1).wait_recv()
        a_c(kind, z_size - 1, 1).start()
    for kind in range(3):
        f_x(kind, 0).start()
        f_c(kind, 0, 0).start()
    tok_y_in.wait_recv()
    own_q.wait()
    own_o.wait()
    for kind in (0, 1):
        for step in range(z_size):
            for far in range(2):
                a_c_in(kind, step, far).wait_recv()

    gains = kv_w[:, 2 * head :].astype(jnp.float32).T[:8, :]
    gain_ref[...] = gains

    def norm_rows(index, carry):
        at = pl.ds(pl.multiple_of(index * 32, 32), 32)
        values = tok[at, :].astype(jnp.float32)
        scale = lax.rsqrt(jnp.mean(values * values, axis=-1, keepdims=True) + epsilon)
        n1_ref[at, :] = (values * scale * gain_ref[0:1, :]).astype(jnp.bfloat16)
        return carry

    lax.fori_loop(0, 2 * own // 32, norm_rows, 0)
    table = (table_ref[0], table_ref[1])
    key_ref[...] = spin(dot_nn(n1_ref[...], kv_w[:, :head]), table).astype(jnp.bfloat16)
    val_ref[...] = dot_nn(n1_ref[...], kv_w[:, head : 2 * head]).astype(jnp.bfloat16)
    head_scale = head ** (-0.5)

    def attend(index, carry):
        cols = pl.ds(pl.multiple_of(index * head, head), head)
        query = dot_nn(n1_ref[...], q_w[:, cols])
        rotated = (spin(query, table) * head_scale).astype(jnp.bfloat16)
        rot_ref[:, cols] = rotated
        probs = head_probs(rotated, key_ref[...], allow_ref[...]).astype(jnp.bfloat16)
        att_ref[:, cols] = dot_nn(probs, val_ref[...]).astype(jnp.bfloat16)
        return carry

    lax.fori_loop(0, att_ref.shape[1] // head, attend, 0)
    for step in range(z_size):
        for far in range(2):
            a_c_in(2, step, far).wait_recv()
    saves = [
        local(kv_w, kv_out),
        local(q_w, wq_out),
        local(o_w, wo_out),
    ]
    span = width // 4

    def project(index, carry):
        cols = pl.ds(pl.multiple_of(index * span, span), span)
        part[:, cols] = matmul_nt(att_ref[...], o_w[cols, :]).astype(jnp.bfloat16)
        return carry

    lax.fori_loop(0, 4, project, 0)
    part_out.start()

    for step in range(1, z_size):
        if step == 1:
            part_out.wait_recv()

            def middle(index, carry):
                at = pl.ds(pl.multiple_of(index * 32, 32), 32)
                there = pl.ds(pl.multiple_of(me_y * own + index * 32, 32), 32)
                values = (
                    tok_ref[at, :].astype(jnp.float32)
                    + part[there, :].astype(jnp.float32)
                    + part_y[at, :].astype(jnp.float32)
                )
                mid_ref[at, :] = values
                scale = lax.rsqrt(jnp.mean(values * values, axis=-1, keepdims=True) + epsilon)
                n2_ref[at, :] = (values * scale * gain_ref[1:2, :]).astype(jnp.bfloat16)
                return carry

            lax.fori_loop(0, own // 32, middle, 0)
        kind = step - 1
        for step_from in (1, 3, 2):
            for copy in f_z_in(kind, step_from):
                copy.wait_recv()
            f_x(kind, step_from).start()
            f_c(kind, step_from, 0).start()
        d_z_in(step).wait_recv()
        if step < z_size - 1:
            d_z(step).start()
        d_y(step).start()
    for kind in range(3):
        for step in (0, 1, 3, 2):
            f_x_in(kind, step).wait_recv()
            f_c(kind, step, 1).start()
    for kind in range(3):
        for step in range(z_size):
            for far in range(2):
                f_c_in(kind, step, far).wait_recv()
    for step in range(z_size):
        d_y_in(step).wait_recv()

    kv_y.wait_send()
    tok_y.wait_send()
    part_out.wait_send()
    own_d.wait()
    for copy in saves:
        copy.wait()
    for step in range(z_size):
        d_y(step).wait_send()
        if step < z_size - 1:
            d_z(step).wait_send()
        for kind in range(3):
            if step < z_size - 1:
                a_z(kind, step).wait_send()
            if step:
                for copy in f_z(kind, step):
                    copy.wait_send()
            a_x(kind, step).wait_send()
            f_x(kind, step).wait_send()
            for far in range(2):
                a_c(kind, step, far).wait_send()
                f_c(kind, step, far).wait_send()


def pre_call(tokens, kv_gains, table, allowed, cotangent, w_query, w_out, ffn):
    z_size = lax.axis_size("z")
    own, width = tokens.shape
    seq = 2 * own
    rows, cols = w_query.shape
    head = table.shape[2] * 2
    units = ragged_split(ffn[0].shape[1], z_size)[1]
    low = lambda *dims: jax.ShapeDtypeStruct(dims, jnp.bfloat16)
    full = lambda *dims: jax.ShapeDtypeStruct(dims, jnp.float32)
    dma = lambda *lead: pltpu.SemaphoreType.DMA(lead)
    vmem = pl.BlockSpec(memory_space=pltpu.VMEM)
    hbm = pl.BlockSpec(memory_space=pl.ANY)
    wide = lambda *lead: pltpu.VMEM((*lead, width), jnp.bfloat16)
    return pl.pallas_call(
        functools.partial(pre_kernel, z_size),
        out_shape=(
            low(seq, width),
            low(seq, cols),
            low(seq, head),
            low(seq, head),
            low(seq, cols),
            full(own, width),
            low(own, width),
            full(8, width),
            low(width, kv_gains.shape[1]),
            low(width, cols),
            low(width, cols),
            low(3, width, units),
            low(z_size, seq, width),
        ),
        in_specs=[vmem] * 4 + [hbm] * 6,
        out_specs=(vmem,) * 8 + (hbm,) * 5,
        scratch_shapes=[
            pltpu.VMEM((width, kv_gains.shape[1]), jnp.bfloat16),
            pltpu.VMEM((width, cols), jnp.bfloat16),
            pltpu.VMEM((width, cols), jnp.bfloat16),
            wide(seq),
            wide(seq),
            wide(own),
            dma(3),
            dma(3),
            dma(3, z_size),
            dma(3, z_size),
            dma(3, z_size),
            dma(3, z_size),
            dma(3, 2 * z_size),
            dma(3, 2 * z_size),
            dma(3, z_size, 2),
            dma(3, z_size, 2),
            dma(3, z_size),
            dma(3, z_size),
            dma(3, 2 * z_size),
            dma(3, 2 * z_size),
            dma(z_size),
            dma(z_size),
            dma(z_size),
            dma(z_size),
            dma(16),
        ],
        compiler_params=pltpu.CompilerParams(
            collective_id=1, has_side_effects=True, vmem_limit_bytes=VMEM_BYTES
        ),
        cost_estimate=pl.CostEstimate(
            flops=8 * seq * width * cols,
            bytes_accessed=8 * width * (cols + units),
            transcendentals=seq * seq * cols // head,
        ),
    )(tokens, kv_gains, table, allowed, cotangent, w_query, w_out, *ffn)


FF_SPLIT = 4


def shards_general(
    tokens,
    segments,
    positions,
    cotangent,
    attn_gain,
    ffn_gain,
    w_kv,
    w_query,
    w_out,
    w_gate,
    w_up,
    w_down,
):
    everywhere = ("z", "xc", "mp")
    dp = ("z", "xc")
    z_size = lax.axis_size("z")
    xc_size = lax.axis_size("xc")
    gains = lax.all_gather(
        jnp.stack([attn_gain, ffn_gain], axis=1), everywhere, axis=0, tiled=True
    ).astype(jnp.float32)
    gain_one, gain_two = gains[:, 0], gains[:, 1]
    kv_weight = lax.all_gather(w_kv, everywhere, axis=0, tiled=True)
    head_dim = kv_weight.shape[1] // 2
    width = tokens.shape[1]
    seq_len = segments.shape[0]
    heads_here = w_query.shape[1] // head_dim
    scale = head_dim ** (-0.5)
    cosine, sine = rotary_angles(positions, head_dim)
    inputs_f = tokens.astype(jnp.float32)
    tokens_all = lax.all_gather(tokens, "mp", axis=0, tiled=True)
    normed_one = norm_gain(tokens_all.astype(jnp.float32), gain_one).astype(jnp.bfloat16)
    query_weight = lax.all_gather(w_query, dp, axis=0, tiled=True)
    out_weight = lax.all_gather(w_out, dp, axis=0, tiled=True)

    rows = w_gate.shape[0]
    unit = w_gate.shape[1] // z_size
    units = -(-unit // TILE) * TILE

    def spread(weight):
        pieces = weight.reshape(rows, z_size, unit).transpose(1, 0, 2)
        pieces = jnp.pad(pieces, ((0, 0), (0, 0), (0, units - unit)))
        pieces = lax.all_to_all(pieces, "z", split_axis=0, concat_axis=0, tiled=True)
        return lax.all_gather(pieces, "xc", axis=1, tiled=False).reshape(width, units)

    ffn_weights = jnp.stack([spread(w_gate), spread(w_up), spread(w_down)])
    grad_all = lax.all_gather(cotangent, ("z", "mp"), axis=0, tiled=True)
    grad_all = grad_all.reshape(z_size, seq_len, width)

    query = jnp.dot(normed_one, query_weight, preferred_element_type=jnp.float32).reshape(
        seq_len, heads_here, head_dim
    )
    rotated = (rotate(query, cosine[:, None], sine[:, None]) * scale).astype(jnp.bfloat16)
    keyval = jnp.dot(normed_one, kv_weight, preferred_element_type=jnp.float32)
    keys = rotate(keyval[:, :head_dim], cosine, sine).astype(jnp.bfloat16)
    values = keyval[:, head_dim:].astype(jnp.bfloat16)
    allowed = block_allowed(segments, 0, seq_len)
    scores = jnp.einsum("thd,sd->hts", rotated, keys, preferred_element_type=jnp.float32)
    scores = jnp.where(allowed[None], scores, masked_score)
    row_max = jnp.max(scores, axis=-1, keepdims=True)
    weights = jnp.exp(scores - row_max)
    probs = weights / jnp.sum(weights, axis=-1, keepdims=True)
    probs_low = probs.astype(jnp.bfloat16)
    attn_vals = (
        jnp.einsum("hts,sd->thd", probs_low, values, preferred_element_type=jnp.float32)
        .reshape(seq_len, heads_here * head_dim)
        .astype(jnp.bfloat16)
    )
    mid = inputs_f + lax.psum_scatter(
        matmul_nt(attn_vals, out_weight).astype(jnp.bfloat16),
        "mp",
        scatter_dimension=0,
        tiled=True,
    ).astype(jnp.float32)
    normed_two = norm_gain(mid, gain_two).astype(jnp.bfloat16)
    grad_normed_two, mixed_sum, weight_parts = ffn_call(normed_two, grad_all, ffn_weights, 0)
    mixed = (mid + mixed_sum).astype(jnp.bfloat16)

    def collect(part):
        pieces = part.reshape(z_size, xc_size, rows, units).transpose(1, 0, 2, 3)
        pieces = pieces.reshape(xc_size * z_size * rows, units)
        pieces = lax.psum_scatter(pieces, "xc", scatter_dimension=0, tiled=True)
        pieces = pieces.reshape(z_size, rows, units)
        pieces = lax.all_to_all(pieces, "z", split_axis=0, concat_axis=0, tiled=True)
        pieces = pieces[:, :, :unit]
        return pieces.transpose(1, 0, 2).reshape(rows, z_size * unit).astype(jnp.float32)

    w_gate_grad, w_up_grad, w_down_grad = [collect(weight_parts[kind]) for kind in range(3)]

    norm_pull_two = jax.vjp(norm_gain, mid, gain_two)[1]
    grad_mid_norm, grad_gain_two = norm_pull_two(grad_normed_two)
    grad_mid = cotangent.astype(jnp.float32) + grad_mid_norm
    grad_mid_all = lax.all_gather(grad_mid.astype(jnp.bfloat16), "mp", axis=0, tiled=True)
    grad_vals = (
        jnp.dot(grad_mid_all, out_weight, preferred_element_type=jnp.float32)
        .astype(jnp.bfloat16)
        .reshape(seq_len, heads_here, head_dim)
    )
    grad_probs = jnp.einsum("thd,sd->hts", grad_vals, values, preferred_element_type=jnp.float32)
    delta = jnp.sum(probs * grad_probs, axis=-1, keepdims=True)
    grad_scores = (probs * (grad_probs - delta)).astype(jnp.bfloat16)
    grad_rot = jnp.einsum("hts,sd->thd", grad_scores, keys, preferred_element_type=jnp.float32)
    key_sum = jnp.einsum("hts,thd->sd", grad_scores, rotated, preferred_element_type=jnp.float32)
    value_sum = jnp.einsum("hts,thd->sd", probs_low, grad_vals, preferred_element_type=jnp.float32)
    grad_query = (
        (unrotate(grad_rot, cosine[:, None], sine[:, None]) * scale)
        .reshape(seq_len, heads_here * head_dim)
        .astype(jnp.bfloat16)
    )
    grad_kv = jnp.concatenate([unrotate(key_sum, cosine, sine), value_sum], axis=1).astype(
        jnp.bfloat16
    )
    grad_normed_one = lax.psum_scatter(
        (matmul_nt(grad_query, query_weight) + matmul_nt(grad_kv, kv_weight)).astype(jnp.bfloat16),
        "mp",
        scatter_dimension=0,
        tiled=True,
    ).astype(jnp.float32)
    norm_pull_one = jax.vjp(norm_gain, inputs_f, gain_one)[1]
    grad_input_norm, grad_gain_one = norm_pull_one(grad_normed_one)
    tokens_grad = (grad_mid + grad_input_norm).astype(jnp.bfloat16)

    w_query_grad = lax.psum_scatter(
        matmul_tn(normed_one, grad_query).astype(jnp.bfloat16), dp, scatter_dimension=0, tiled=True
    ).astype(jnp.float32)
    w_out_grad = lax.psum_scatter(
        matmul_tn(grad_mid_all, attn_vals).astype(jnp.bfloat16), dp, scatter_dimension=0, tiled=True
    ).astype(jnp.float32)
    small = jnp.concatenate(
        [matmul_tn(normed_one, grad_kv), grad_gain_one[:, None], grad_gain_two[:, None]], axis=1
    )
    small = lax.psum_scatter(small, everywhere, scatter_dimension=0, tiled=True)
    kv_grad = small[:, : 2 * head_dim]
    return (
        mixed,
        tokens_grad,
        small[:, 2 * head_dim],
        small[:, 2 * head_dim + 1],
        kv_grad,
        w_query_grad,
        w_out_grad,
        w_gate_grad,
        w_up_grad,
        w_down_grad,
    )


def shards_fast(
    tokens,
    segments,
    positions,
    cotangent,
    attn_gain,
    ffn_gain,
    w_kv,
    w_query,
    w_out,
    w_gate,
    w_up,
    w_down,
):
    everywhere = ("z", "x", "c", "mp")
    dp = ("z", "x", "c")
    z_size = lax.axis_size("z")
    head_dim = w_kv.shape[1] // 2
    width = tokens.shape[1]
    seq_len = segments.shape[0]
    heads_here = w_query.shape[1] // head_dim
    scale = head_dim ** (-0.5)
    cosine, sine = rotary_angles(positions, head_dim)
    table = jnp.stack(
        [
            jnp.concatenate([cosine, cosine], axis=1),
            jnp.concatenate([-sine, sine], axis=1),
        ]
    )
    allowed = block_allowed(segments, 0, seq_len)
    kv_gains = jnp.concatenate(
        [w_kv, attn_gain[:, None], ffn_gain[:, None], jnp.zeros((w_kv.shape[0], 126), w_kv.dtype)],
        axis=1,
    )
    inputs_f = tokens.astype(jnp.float32)
    (
        normed_one,
        rotated_flat,
        keys,
        values,
        attn_vals,
        mid,
        normed_two,
        gains,
        kv_weight,
        query_weight,
        out_weight,
        ffn_weights,
        grad_all,
    ) = pre_call(
        tokens,
        kv_gains,
        table,
        allowed.astype(jnp.float32),
        cotangent,
        w_query,
        w_out,
        (w_gate, w_up, w_down),
    )
    kv_weight = kv_weight[:, : 2 * head_dim]
    gain_one, gain_two = gains[0], gains[1]
    rotated = rotated_flat.reshape(seq_len, heads_here, head_dim)

    rows = w_gate.shape[0]
    main, units = ragged_split(w_gate.shape[1], z_size)
    grad_normed_two, mixed_sum, weight_parts = ffn_call(normed_two, grad_all, ffn_weights, main)
    mixed = (mid + mixed_sum).astype(jnp.bfloat16)

    def collect(part):
        pieces = part.reshape(z_size, 4, rows, units).transpose(1, 0, 2, 3)
        pieces = pieces.reshape(4 * z_size * rows, units)
        pieces = lax.psum_scatter(pieces, ("x", "c"), scatter_dimension=0, tiled=True)
        pieces = pieces.reshape(z_size, rows, units)
        pieces = lax.all_to_all(pieces, "z", split_axis=0, concat_axis=0, tiled=True)
        pieces = pieces.transpose(1, 0, 2).astype(jnp.float32)
        tails = pieces[:, :, main:].reshape(rows, z_size // 2, 2, 128).sum(axis=2)
        return jnp.concatenate(
            [pieces[:, :, :main].reshape(rows, z_size * main), tails.reshape(rows, -1)], axis=1
        )

    w_gate_grad, w_up_grad, w_down_grad = [collect(weight_parts[kind]) for kind in range(3)]

    norm_pull_two = jax.vjp(norm_gain, mid, gain_two)[1]
    grad_mid_norm, grad_gain_two = norm_pull_two(grad_normed_two)
    grad_mid = cotangent.astype(jnp.float32) + grad_mid_norm
    grad_mid_all = lax.all_gather(grad_mid.astype(jnp.bfloat16), "mp", axis=0, tiled=True)
    grad_vals = (
        jnp.dot(grad_mid_all, out_weight, preferred_element_type=jnp.float32)
        .astype(jnp.bfloat16)
        .reshape(seq_len, heads_here, head_dim)
    )
    scores = jnp.einsum("thd,sd->hts", rotated, keys, preferred_element_type=jnp.float32)
    scores = jnp.where(allowed[None], scores, masked_score)
    weights = jnp.exp(scores - jnp.max(scores, axis=-1, keepdims=True))
    probs = weights / jnp.sum(weights, axis=-1, keepdims=True)
    probs_low = probs.astype(jnp.bfloat16)
    grad_probs = jnp.einsum("thd,sd->hts", grad_vals, values, preferred_element_type=jnp.float32)
    delta = jnp.sum(probs * grad_probs, axis=-1, keepdims=True)
    grad_scores = (probs * (grad_probs - delta)).astype(jnp.bfloat16)
    grad_rot = jnp.einsum("hts,sd->thd", grad_scores, keys, preferred_element_type=jnp.float32)
    key_sum = jnp.einsum("hts,thd->sd", grad_scores, rotated, preferred_element_type=jnp.float32)
    value_sum = jnp.einsum("hts,thd->sd", probs_low, grad_vals, preferred_element_type=jnp.float32)
    grad_query = (
        (unrotate(grad_rot, cosine[:, None], sine[:, None]) * scale)
        .reshape(seq_len, heads_here * head_dim)
        .astype(jnp.bfloat16)
    )
    grad_kv = jnp.concatenate([unrotate(key_sum, cosine, sine), value_sum], axis=1).astype(
        jnp.bfloat16
    )
    grad_normed_one = lax.psum_scatter(
        (matmul_nt(grad_query, query_weight) + matmul_nt(grad_kv, kv_weight)).astype(jnp.bfloat16),
        "mp",
        scatter_dimension=0,
        tiled=True,
    ).astype(jnp.float32)
    norm_pull_one = jax.vjp(norm_gain, inputs_f, gain_one)[1]
    grad_input_norm, grad_gain_one = norm_pull_one(grad_normed_one)
    tokens_grad = (grad_mid + grad_input_norm).astype(jnp.bfloat16)

    w_query_grad = lax.psum_scatter(
        matmul_tn(normed_one, grad_query).astype(jnp.bfloat16), dp, scatter_dimension=0, tiled=True
    ).astype(jnp.float32)
    w_out_grad = lax.psum_scatter(
        matmul_tn(grad_mid_all, attn_vals).astype(jnp.bfloat16), dp, scatter_dimension=0, tiled=True
    ).astype(jnp.float32)
    small = jnp.concatenate(
        [matmul_tn(normed_one, grad_kv), grad_gain_one[:, None], grad_gain_two[:, None]], axis=1
    )
    small = lax.psum_scatter(small, everywhere, scatter_dimension=0, tiled=True)
    kv_grad = small[:, : 2 * head_dim]
    return (
        mixed,
        tokens_grad,
        small[:, 2 * head_dim],
        small[:, 2 * head_dim + 1],
        kv_grad,
        w_query_grad,
        w_out_grad,
        w_gate_grad,
        w_up_grad,
        w_down_grad,
    )


def solution(mesh):
    dp_size, mp_size = mesh.shape["dp"], mesh.shape["mp"]
    if dp_size == 4 * FF_SPLIT and mp_size == 2:
        body, dp = shards_fast, ("z", "x", "c")
        sizes = (FF_SPLIT, 2, 2, mp_size)
    else:
        body, dp = shards_general, ("z", "xc")
        sizes = (FF_SPLIT, dp_size // FF_SPLIT, mp_size)
    all_axes = (*dp, "mp")
    fine = jax.sharding.Mesh(mesh.devices.reshape(sizes), all_axes)
    in_specs = (
        P(all_axes, None),
        P(dp),
        P(dp),
        P(all_axes, None),
        P(all_axes),
        P(all_axes),
        P(all_axes, None),
        P(dp, "mp"),
        P(dp, "mp"),
        P(dp, "mp"),
        P(dp, "mp"),
        P(dp, "mp"),
    )
    out_specs = (
        P(all_axes, None),
        P(all_axes, None),
        P(all_axes),
        P(all_axes),
        P(all_axes, None),
        P(dp, "mp"),
        P(dp, "mp"),
        P(dp, "mp"),
        P(dp, "mp"),
        P(dp, "mp"),
    )
    return jax.shard_map(body, mesh=fine, in_specs=in_specs, out_specs=out_specs, check_vma=False)
```

```python
import functools

import jax
import jax.numpy as jnp
from jax import lax
from jax.experimental import pallas as pl
from jax.experimental.pallas import tpu as pltpu
from jax.sharding import PartitionSpec as P

WINDOW = 2048


epsilon = 1e-06
rope_base = 10000.0
masked_score = -1e30
VMEM_BYTES = 65_000_000


def norm_gain(values, gain):
    return values * lax.rsqrt(jnp.mean(values * values, axis=-1, keepdims=True) + epsilon) * gain


def rotary_angles(positions, head_width):
    quarter = head_width // 4
    freqs = rope_base ** (-jnp.arange(quarter).astype(jnp.float32) / quarter)
    phase = positions.astype(jnp.float32)[:, None] * freqs[None, :]
    return (jnp.cos(phase), jnp.sin(phase))


def rotate(values, cosine, sine):
    quarter = cosine.shape[-1]
    first_half = values[..., :quarter]
    second_half = values[..., quarter : 2 * quarter]
    return jnp.concatenate(
        [
            first_half * cosine - second_half * sine,
            second_half * cosine + first_half * sine,
            values[..., 2 * quarter :],
        ],
        axis=-1,
    )


def unrotate(values, cosine, sine):
    quarter = cosine.shape[-1]
    first_half = values[..., :quarter]
    second_half = values[..., quarter : 2 * quarter]
    return jnp.concatenate(
        [
            first_half * cosine + second_half * sine,
            second_half * cosine - first_half * sine,
            values[..., 2 * quarter :],
        ],
        axis=-1,
    )


def gelu_product(gate, up_proj):
    return jax.nn.gelu(gate, approximate=True) * up_proj


def matmul_nt(left, right):
    return lax.dot_general(
        left, right, (((1,), (1,)), ((), ())), preferred_element_type=jnp.float32
    )


def matmul_tn(left, right):
    return lax.dot_general(
        left, right, (((0,), (0,)), ((), ())), preferred_element_type=jnp.float32
    )


def block_allowed(segments, first_row, rows):
    seq_len = segments.shape[0]
    query_rows = first_row + jnp.arange(rows)
    key_rows = jnp.arange(seq_len)
    return (
        (segments[:, None] == segments[None, :])
        & (key_rows[None, :] <= query_rows[:, None])
        & (query_rows[:, None] - key_rows[None, :] < WINDOW)
    )


MESH_ID = pl.DeviceIdType.MESH
GELU_A = 0.7978845608028654
GELU_B = 0.044715
TILE = 256


def remote(src, dst, send_sem, recv_sem, where):
    return pltpu.make_async_remote_copy(
        src_ref=src,
        dst_ref=dst,
        send_sem=send_sem,
        recv_sem=recv_sem,
        device_id=where,
        device_id_type=MESH_ID,
    )


def dot_nn(left, right):
    return lax.dot_general(
        left, right, (((1,), (0,)), ((), ())), preferred_element_type=jnp.float32
    )


def gelu_parts(gate):
    square = gate * gate
    bend = jnp.tanh(GELU_A * gate * (1.0 + GELU_B * square))
    half = 0.5 * (1.0 + bend)
    slope = half + 0.5 * gate * (1.0 - bend * bend) * GELU_A * (1.0 + 3.0 * GELU_B * square)
    return gate * half, slope


def add_rows(first, rest, out, count):
    def body(index, carry):
        step = pl.ds(pl.multiple_of(index * 32, 32), 32)
        total = first[step, :].astype(jnp.float32)
        for other in rest:
            total = total + other[step, :].astype(jnp.float32)
        out[step, :] = total.astype(out.dtype)
        return carry

    lax.fori_loop(0, count // 32, body, 0)


def ffn_kernel(
    z_size,
    main,
    own_ref,
    dy_hbm,
    w_hbm,
    gn_ref,
    mix_hbm,
    grads_hbm,
    n2,
    dy,
    w3,
    h3,
    left_t,
    gn_part,
    mix_buf,
    gn_y,
    gn_z,
    gn_s,
    c_in,
    x_in,
    load_sem,
    mix_sem,
    ag_y_send,
    ag_y_recv,
    ag_z_send,
    ag_z_recv,
    rs_y_send,
    rs_y_recv,
    rs_z_send,
    rs_z_recv,
    c_send,
    c_recv,
    x_send,
    x_recv,
    z_send,
    z_recv,
    out_sem,
):
    own = own_ref.shape[0]
    width = own_ref.shape[1]
    units = w3.shape[2]
    rows = c_in.shape[3]
    me_y, me_z = lax.axis_index("mp"), lax.axis_index("z")
    me_x, me_c = lax.axis_index("x"), lax.axis_index("c")
    mine = pl.ds(pl.multiple_of(me_y * own, own), own)
    theirs = pl.ds(pl.multiple_of((1 - me_y) * own, own), own)
    to_y, to_x, to_c = {"mp": 1 - me_y}, {"x": 1 - me_x}, {"c": 1 - me_c}

    def ahead(step):
        return lax.rem(me_z + step, z_size)

    def to_z(step):
        return {"z": ahead(step)}

    def row_block(z_at, x_at, c_at):
        return pl.ds(pl.multiple_of(((z_at * 2 + x_at) * 2 + c_at) * rows, rows), rows)

    loads = []
    for index in range(z_size):
        loads.append(pltpu.make_async_copy(dy_hbm.at[index], dy.at[index], load_sem.at[index]))
    for index in range(3):
        loads.append(
            pltpu.make_async_copy(w_hbm.at[index], w3.at[index], load_sem.at[z_size + index])
        )
    for load in loads:
        load.start()

    barrier = pltpu.get_barrier_semaphore()
    peers = [to_y, to_x, to_c] + [to_z(step) for step in range(1, z_size)]
    for where in peers:
        pl.semaphore_signal(barrier, inc=1, device_id=where, device_id_type=MESH_ID)
    pl.semaphore_wait(barrier, len(peers))

    def ag_y(index):
        src = own_ref if index == 0 else n2.at[index, mine]
        return remote(src, n2.at[index, mine], ag_y_send.at[index], ag_y_recv.at[index], to_y)

    def ag_y_in(index):
        block = n2.at[index, theirs]
        return remote(block, block, ag_y_send.at[index], ag_y_recv.at[index], to_y)

    def ag_z(index):
        src = own_ref if index == 0 else n2.at[index, mine]
        return remote(
            src, n2.at[index + 1, mine], ag_z_send.at[index], ag_z_recv.at[index + 1], to_z(1)
        )

    def ag_z_in(index):
        block = n2.at[index, mine]
        return remote(block, block, ag_z_send.at[0], ag_z_recv.at[index], to_z(1))

    def forward(index):
        ag_z_in(index).wait_recv()
        if index < z_size - 1:
            ag_z(index).start()
        ag_y(index).start()

    ag_y(0).start()
    ag_z(0).start()
    n2[0, mine, :] = own_ref[...]

    mix_copies = []

    def chunk(index):
        ag_y_in(index).wait_recv()
        if index >= 2:
            mix_copies[index - 2].wait()
        rows_at = pl.ds(index * 2 * own, 2 * own)

        def up_tile(tile, carry):
            cols = pl.ds(pl.multiple_of(tile * TILE, TILE), TILE)
            normed = n2[index]
            gate = dot_nn(normed, w3[0, :, cols])
            up_proj = dot_nn(normed, w3[1, :, cols])
            grad_hidden = dot_nn(dy[index], w3[2, :, cols])
            act, slope = gelu_parts(gate)
            at = lax.broadcasted_iota(jnp.int32, (1, TILE), 1) + tile * TILE
            low_at = main + 64 * lax.rem(me_z, 2)
            keep = (at < main) | ((at >= low_at) & (at < low_at + 64))
            act = jnp.where(keep, act, 0.0)
            slope = jnp.where(keep, slope, 0.0)
            h3[0, rows_at, cols] = (grad_hidden * up_proj * slope).astype(jnp.bfloat16)
            h3[1, rows_at, cols] = (grad_hidden * act).astype(jnp.bfloat16)
            h3[2, rows_at, cols] = (act * up_proj).astype(jnp.bfloat16)
            return carry

        lax.fori_loop(0, units // TILE, up_tile, 0)

        def down_tile(tile, carry):
            cols = pl.ds(pl.multiple_of(tile * TILE, TILE), TILE)
            gn_part[index, :, cols] = (
                matmul_nt(h3[0, rows_at, :], w3[0, cols, :])
                + matmul_nt(h3[1, rows_at, :], w3[1, cols, :])
            ).astype(jnp.bfloat16)
            mix_buf[index % 2, :, cols] = matmul_nt(h3[2, rows_at, :], w3[2, cols, :]).astype(
                jnp.bfloat16
            )
            return carry

        lax.fori_loop(0, width // TILE, down_tile, 0)
        copy = pltpu.make_async_copy(mix_buf.at[index % 2], mix_hbm.at[index], mix_sem.at[index])
        copy.start()
        mix_copies.append(copy)

    def rs_y(index):
        return remote(
            gn_part.at[index, theirs], gn_y.at[index], rs_y_send.at[index], rs_y_recv.at[index], to_y
        )

    def rs_z(index):
        return remote(
            gn_s.at[index - 1],
            gn_z.at[index - 1],
            rs_z_send.at[index],
            rs_z_recv.at[index - 1],
            to_z(1),
        )

    def rs_step(index):
        rs_y(index).wait_recv()
        slot = (index - 2) % z_size
        if index != 1:
            remote(
                gn_s.at[slot], gn_z.at[slot], rs_z_send.at[1], rs_z_recv.at[slot], to_z(1)
            ).wait_recv()

        def add_tile(tile, carry):
            cols = pl.ds(pl.multiple_of(tile * TILE, TILE), TILE)
            total = gn_part[index, mine, cols].astype(jnp.float32) + gn_y[index, :, cols].astype(
                jnp.float32
            )
            if index != 1:
                total = total + gn_z[slot, :, cols].astype(jnp.float32)
            if index == 0:
                gn_ref[:, cols] = total
            else:
                gn_s[index - 1, :, cols] = total.astype(jnp.bfloat16)
            return carry

        lax.fori_loop(0, width // TILE, add_tile, 0)
        if index != 0:
            rs_z(index).start()

    span = width // z_size

    def grads(step):
        at = pl.ds(pl.multiple_of(ahead(step) * span, 128), span)
        for kinds, source in (((0, 1), n2), ((2,), dy)):
            left_t[...] = source[:, :, at].reshape(z_size * 2 * own, span).T
            for kind in kinds:

                def tile_body(tile, carry, kind=kind):
                    cols = pl.ds(pl.multiple_of(tile * TILE, TILE), TILE)
                    w3[kind, at, cols] = dot_nn(left_t[...], h3[kind, :, cols]).astype(jnp.bfloat16)
                    return carry

                lax.fori_loop(0, units // TILE, tile_body, 0)
        for far in (1, 0):
            for kind in range(3):
                over_c(kind, step, far).start()

    def over_c(kind, step, far):
        x_at = 1 - me_x if far else me_x
        return remote(
            w3.at[kind, row_block(ahead(step), x_at, 1 - me_c)],
            c_in.at[kind, step, far],
            c_send.at[kind, step, far],
            c_recv.at[kind, step, far],
            to_c,
        )

    def over_x(kind, step):
        return remote(
            w3.at[kind, row_block(ahead(step), 1 - me_x, me_c)],
            x_in.at[kind, step],
            x_send.at[kind, step],
            x_recv.at[kind, step],
            to_x,
        )

    def over_z(kind, step):
        return remote(
            w3.at[kind, row_block(ahead(step), me_x, me_c)],
            grads_hbm.at[kind, step],
            z_send.at[kind, step],
            z_recv.at[kind, step],
            to_z(step),
        )

    def x_stage(step):
        for kind in range(3):
            over_c(kind, step, 1).wait_recv()
            block = w3.at[kind, row_block(ahead(step), 1 - me_x, me_c)]
            add_rows(block, [c_in.at[kind, step, 1]], block, rows)
            over_x(kind, step).start()

    own_out = []

    def z_stage(step):
        for kind in range(3):
            over_c(kind, step, 0).wait_recv()
            over_x(kind, step).wait_recv()
            block = w3.at[kind, row_block(ahead(step), me_x, me_c)]
            add_rows(block, [c_in.at[kind, step, 0], x_in.at[kind, step]], block, rows)
            if step:
                over_z(kind, step).start()
            else:
                copy = pltpu.make_async_copy(block, grads_hbm.at[kind, 0], out_sem.at[kind])
                copy.start()
                own_out.append(copy)

    forward(1)
    for load in loads:
        load.wait()
    chunk(0)
    rs_y(0).start()
    forward(2)
    chunk(1)
    rs_y(1).start()
    forward(3)
    chunk(2)
    rs_y(2).start()
    rs_step(1)
    chunk(3)
    rs_y(3).start()
    rs_step(2)
    grads(1)
    rs_step(3)
    grads(2)
    x_stage(1)
    rs_step(0)
    grads(3)
    x_stage(2)
    grads(0)
    x_stage(3)
    x_stage(0)
    z_stage(1)
    z_stage(2)
    z_stage(3)
    z_stage(0)

    for copy in mix_copies[2:] + own_out:
        copy.wait()
    for index in range(z_size):
        ag_y(index).wait_send()
        rs_y(index).wait_send()
        if index < z_size - 1:
            ag_z(index).wait_send()
        if index:
            rs_z(index).wait_send()
        for kind in range(3):
            over_c(kind, index, 0).wait_send()
            over_c(kind, index, 1).wait_send()
            over_x(kind, index).wait_send()
            if index:
                over_z(kind, index).wait()


def ffn_call(normed, grad_all, weights, rows, main):
    z_size = lax.axis_size("z")
    own, width = normed.shape
    units = weights.shape[2]
    pair = 2 * own
    wide = lambda *lead: pltpu.VMEM((*lead, width), jnp.bfloat16)
    dma = lambda *lead: pltpu.SemaphoreType.DMA(lead)
    vmem = pl.BlockSpec(memory_space=pltpu.VMEM)
    hbm = pl.BlockSpec(memory_space=pl.ANY)
    return pl.pallas_call(
        functools.partial(ffn_kernel, z_size, main),
        out_shape=(
            jax.ShapeDtypeStruct((own, width), jnp.float32),
            jax.ShapeDtypeStruct((z_size, pair, width), jnp.bfloat16),
            jax.ShapeDtypeStruct((3, z_size, rows, units), jnp.bfloat16),
        ),
        in_specs=[vmem, hbm, hbm],
        out_specs=(vmem, hbm, hbm),
        scratch_shapes=[
            wide(z_size, pair),
            wide(z_size, pair),
            pltpu.VMEM(weights.shape, jnp.bfloat16),
            pltpu.VMEM((3, z_size * pair, units), jnp.bfloat16),
            pltpu.VMEM((width // z_size, z_size * pair), jnp.bfloat16),
            wide(z_size, pair),
            wide(2, pair),
            wide(z_size, own),
            wide(z_size - 1, own),
            wide(z_size - 1, own),
            pltpu.VMEM((3, z_size, 2, rows, units), jnp.bfloat16),
            pltpu.VMEM((3, z_size, rows, units), jnp.bfloat16),
            dma(z_size + 3),
            dma(z_size),
            dma(z_size),
            dma(z_size),
            dma(z_size),
            dma(z_size),
            dma(z_size),
            dma(z_size),
            dma(z_size),
            dma(z_size),
            dma(3, z_size, 2),
            dma(3, z_size, 2),
            dma(3, z_size),
            dma(3, z_size),
            dma(3, z_size),
            dma(3, z_size),
            dma(3),
        ],
        compiler_params=pltpu.CompilerParams(
            collective_id=0, has_side_effects=True, vmem_limit_bytes=VMEM_BYTES
        ),
        cost_estimate=pl.CostEstimate(
            flops=18 * z_size * pair * width * units,
            bytes_accessed=4 * weights.size + 12 * z_size * pair * width,
            transcendentals=z_size * pair * units,
        ),
    )(normed, grad_all, weights)


def spin(values, table):
    first = values[:, : values.shape[1] // 2]
    turned = first * table[0] + pltpu.roll(first, first.shape[1] // 2, 1) * table[1]
    return jnp.concatenate([turned, values[:, values.shape[1] // 2 :]], axis=1)


def spin_back(values, table):
    first = values[:, : values.shape[1] // 2]
    turned = first * table[0] - pltpu.roll(first, first.shape[1] // 2, 1) * table[1]
    return jnp.concatenate([turned, values[:, values.shape[1] // 2 :]], axis=1)


def head_probs(rotated, keys, allowed):
    scores = jnp.where(allowed > 0.5, matmul_nt(rotated, keys), masked_score)
    weights = jnp.exp(scores - jnp.max(scores, axis=-1, keepdims=True))
    return weights / jnp.sum(weights, axis=-1, keepdims=True)


def ragged_split(columns, parts):
    main = columns // parts // 128 * 128
    return main, main + 128


def pre_kernel(
    z_size,
    tok_ref,
    kvg_ref,
    table_ref,
    allow_ref,
    cot_hbm,
    wq_hbm,
    wo_hbm,
    wg_hbm,
    wu_hbm,
    wd_hbm,
    n1_ref,
    rot_ref,
    key_ref,
    val_ref,
    att_ref,
    mid_ref,
    n2_ref,
    gain_ref,
    kv_out,
    wq_out,
    wo_out,
    w3_out,
    dy_out,
    kv_w,
    q_w,
    o_w,
    tok,
    part,
    part_y,
    y_send,
    y_recv,
    az_send,
    az_recv,
    ax_send,
    ax_recv,
    ac_send,
    ac_recv,
    fz_send,
    fz_recv,
    fx_send,
    fx_recv,
    fc_send,
    fc_recv,
    dz_send,
    dz_recv,
    dy_send,
    dy_recv,
    local_sem,
):
    me_z, me_x = lax.axis_index("z"), lax.axis_index("x")
    me_c, me_y = lax.axis_index("c"), lax.axis_index("mp")
    own, width = tok_ref.shape
    rows = wq_hbm.shape[0]
    half_rows = kvg_ref.shape[0]
    head = key_ref.shape[1]
    main, units = ragged_split(wg_hbm.shape[1], z_size)
    to_y, to_x, to_c = {"mp": 1 - me_y}, {"x": 1 - me_x}, {"c": 1 - me_c}

    def to_z(step):
        return {"z": lax.rem(me_z + step, z_size)}

    def from_z(step):
        return lax.rem(me_z - step + z_size, z_size)

    def row_block(step, x_at, c_at):
        start = ((from_z(step) * 2 + x_at) * 2 + c_at) * rows
        return pl.ds(pl.multiple_of(start, rows), rows)

    mine = pl.ds(pl.multiple_of(me_y * own, own), own)
    theirs = pl.ds(pl.multiple_of((1 - me_y) * own, own), own)
    bufs = (kv_w, q_w, o_w)
    inputs = (None, wq_hbm, wo_hbm)

    locals_ = []

    def local(src, dst):
        copy = pltpu.make_async_copy(src, dst, local_sem.at[len(locals_)])
        copy.start()
        locals_.append(copy)
        return copy

    here = row_block(0, me_x, me_c)
    own_q = local(wq_hbm, q_w.at[here])
    own_o = local(wo_hbm, o_w.at[here])
    ffn_in = (wg_hbm, wu_hbm, wd_hbm)

    def pieces(target):
        yield pl.ds(pl.multiple_of(target * main, 128), main), pl.ds(0, main)
        tail = (z_size * main) + (target // 2) * 128
        yield pl.ds(pl.multiple_of(tail, 128), 128), pl.ds(main, 128)

    own_f = []
    for kind in range(3):
        for src, dst in pieces(me_z):
            own_f.append(local(ffn_in[kind].at[:, src], w3_out.at[kind, here, dst]))
    own_d = local(cot_hbm, dy_out.at[0, mine])

    barrier = pltpu.get_barrier_semaphore()
    peers = [to_y, to_x, to_c] + [to_z(step) for step in range(1, z_size)]
    for where in peers:
        pl.semaphore_signal(barrier, inc=1, device_id=where, device_id_type=MESH_ID)
    pl.semaphore_wait(barrier, len(peers))

    kv_mine = pl.ds(pl.multiple_of(here.start + me_y * half_rows, half_rows), half_rows)
    kv_theirs = pl.ds(pl.multiple_of(here.start + (1 - me_y) * half_rows, half_rows), half_rows)
    kv_y = remote(kvg_ref, kv_w.at[kv_mine], y_send.at[0], y_recv.at[0], to_y)
    kv_y_in = remote(kvg_ref, kv_w.at[kv_theirs], y_send.at[0], y_recv.at[0], to_y)
    tok_y = remote(tok_ref, tok.at[mine], y_send.at[1], y_recv.at[1], to_y)
    tok_y_in = remote(tok_ref, tok.at[theirs], y_send.at[1], y_recv.at[1], to_y)
    part_out = remote(part.at[theirs], part_y, y_send.at[2], y_recv.at[2], to_y)

    def source(kind, step):
        if step == 0 and kind:
            return inputs[kind]
        return bufs[kind].at[row_block(step, me_x, me_c)]

    def a_z(kind, step):
        return remote(
            source(kind, step),
            bufs[kind].at[row_block(step, me_x, me_c)],
            az_send.at[kind, step],
            az_recv.at[kind, step + 1],
            to_z(1),
        )

    def a_z_in(kind, step):
        block = bufs[kind].at[row_block(step, me_x, me_c)]
        return remote(block, block, az_send.at[kind, 0], az_recv.at[kind, step], to_z(1))

    def a_x(kind, step):
        return remote(
            source(kind, step),
            bufs[kind].at[row_block(step, me_x, me_c)],
            ax_send.at[kind, step],
            ax_recv.at[kind, step],
            to_x,
        )

    def a_x_in(kind, step):
        block = bufs[kind].at[row_block(step, 1 - me_x, me_c)]
        return remote(block, block, ax_send.at[kind, step], ax_recv.at[kind, step], to_x)

    def a_c(kind, step, far):
        x_at = 1 - me_x if far else me_x
        block = bufs[kind].at[row_block(step, x_at, me_c)]
        src = block if far else source(kind, step)
        slot = step + z_size * far
        return remote(src, block, ac_send.at[kind, slot], ac_recv.at[kind, slot], to_c)

    def a_c_in(kind, step, far):
        x_at = 1 - me_x if far else me_x
        block = bufs[kind].at[row_block(step, x_at, 1 - me_c)]
        slot = step + z_size * far
        return remote(block, block, ac_send.at[kind, slot], ac_recv.at[kind, slot], to_c)

    def f_z(kind, step):
        target = lax.rem(me_z + step, z_size)
        return [
            remote(
                ffn_in[kind].at[:, src],
                w3_out.at[kind, here, dst],
                fz_send.at[kind, step, index],
                fz_recv.at[kind, step, index],
                to_z(step),
            )
            for index, (src, dst) in enumerate(pieces(target))
        ]

    def f_z_in(kind, step):
        block = row_block(step, me_x, me_c)
        return [
            remote(
                w3_out.at[kind, block, dst],
                w3_out.at[kind, block, dst],
                fz_send.at[kind, step, index],
                fz_recv.at[kind, step, index],
                to_z(step),
            )
            for index, (_, dst) in enumerate(pieces(me_z))
        ]

    def f_x(kind, step):
        block = w3_out.at[kind, row_block(step, me_x, me_c)]
        return remote(block, block, fx_send.at[kind, step], fx_recv.at[kind, step], to_x)

    def f_x_in(kind, step):
        block = w3_out.at[kind, row_block(step, 1 - me_x, me_c)]
        return remote(block, block, fx_send.at[kind, step], fx_recv.at[kind, step], to_x)

    def f_c(kind, step, far):
        block = w3_out.at[kind, row_block(step, 1 - me_x if far else me_x, me_c)]
        slot = step + z_size * far
        return remote(block, block, fc_send.at[kind, slot], fc_recv.at[kind, slot], to_c)

    def f_c_in(kind, step, far):
        block = w3_out.at[kind, row_block(step, 1 - me_x if far else me_x, 1 - me_c)]
        slot = step + z_size * far
        return remote(block, block, fc_send.at[kind, slot], fc_recv.at[kind, slot], to_c)

    def d_source(step):
        return cot_hbm if step == 0 else dy_out.at[step, mine]

    def d_z(step):
        return remote(
            d_source(step), dy_out.at[step + 1, mine], dz_send.at[step], dz_recv.at[step + 1], to_z(1)
        )

    def d_z_in(step):
        block = dy_out.at[step, mine]
        return remote(block, block, dz_send.at[0], dz_recv.at[step], to_z(1))

    def d_y(step):
        return remote(
            d_source(step), dy_out.at[step, mine], dy_send.at[step], dy_recv.at[step], to_y
        )

    def d_y_in(step):
        block = dy_out.at[step, theirs]
        return remote(block, block, dy_send.at[step], dy_recv.at[step], to_y)

    kv_y.start()
    tok_y.start()
    for kind in (1, 2):
        a_z(kind, 0).start()
        a_x(kind, 0).start()
        a_c(kind, 0, 0).start()
    kv_w[kv_mine, :] = kvg_ref[...]
    tok[mine, :] = tok_ref[...]
    kv_y_in.wait_recv()
    a_z(0, 0).start()
    a_x(0, 0).start()
    a_c(0, 0, 0).start()
    d_y(0).start()
    for step in range(1, z_size):
        for kind in (1, 0, 2):
            a_z_in(kind, step).wait_recv()
            if step < z_size - 1:
                a_z(kind, step).start()
            a_x(kind, step).start()
            a_c(kind, step, 0).start()
        if step == z_size - 2:
            for copy in own_f:
                copy.wait()
            for kind in range(3):
                for away in (1, 3, 2):
                    for copy in f_z(kind, away):
                        copy.start()
            d_z(0).start()
        for kind in (1, 0, 2):
            a_x_in(kind, step - 1).wait_recv()
            a_c(kind, step - 1, 1).start()
    for kind in (1, 0, 2):
        a_x_in(kind, z_size - 1).wait_recv()
        a_c(kind, z_size - 1, 1).start()
    for kind in range(3):
        f_x(kind, 0).start()
        f_c(kind, 0, 0).start()
    tok_y_in.wait_recv()
    own_q.wait()
    own_o.wait()
    for kind in (0, 1):
        for step in range(z_size):
            for far in range(2):
                a_c_in(kind, step, far).wait_recv()

    gains = kv_w[:, 2 * head :].astype(jnp.float32).T[:8, :]
    gain_ref[...] = gains

    def norm_rows(index, carry):
        at = pl.ds(pl.multiple_of(index * 32, 32), 32)
        values = tok[at, :].astype(jnp.float32)
        scale = lax.rsqrt(jnp.mean(values * values, axis=-1, keepdims=True) + epsilon)
        n1_ref[at, :] = (values * scale * gain_ref[0:1, :]).astype(jnp.bfloat16)
        return carry

    lax.fori_loop(0, 2 * own // 32, norm_rows, 0)
    table = (table_ref[0], table_ref[1])
    key_ref[...] = spin(dot_nn(n1_ref[...], kv_w[:, :head]), table).astype(jnp.bfloat16)
    val_ref[...] = dot_nn(n1_ref[...], kv_w[:, head : 2 * head]).astype(jnp.bfloat16)
    head_scale = head ** (-0.5)

    def attend(index, carry):
        cols = pl.ds(pl.multiple_of(index * head, head), head)
        query = dot_nn(n1_ref[...], q_w[:, cols])
        rotated = (spin(query, table) * head_scale).astype(jnp.bfloat16)
        rot_ref[:, cols] = rotated
        probs = head_probs(rotated, key_ref[...], allow_ref[...]).astype(jnp.bfloat16)
        att_ref[:, cols] = dot_nn(probs, val_ref[...]).astype(jnp.bfloat16)
        return carry

    lax.fori_loop(0, att_ref.shape[1] // head, attend, 0)
    for step in range(z_size):
        for far in range(2):
            a_c_in(2, step, far).wait_recv()
    saves = [
        local(kv_w, kv_out),
        local(q_w, wq_out),
        local(o_w, wo_out),
    ]
    span = width // 4

    def project(index, carry):
        cols = pl.ds(pl.multiple_of(index * span, span), span)
        part[:, cols] = matmul_nt(att_ref[...], o_w[cols, :]).astype(jnp.bfloat16)
        return carry

    lax.fori_loop(0, 4, project, 0)
    part_out.start()

    for step in range(1, z_size):
        if step == 1:
            part_out.wait_recv()

            def middle(index, carry):
                at = pl.ds(pl.multiple_of(index * 32, 32), 32)
                there = pl.ds(pl.multiple_of(me_y * own + index * 32, 32), 32)
                values = (
                    tok_ref[at, :].astype(jnp.float32)
                    + part[there, :].astype(jnp.float32)
                    + part_y[at, :].astype(jnp.float32)
                )
                mid_ref[at, :] = values
                scale = lax.rsqrt(jnp.mean(values * values, axis=-1, keepdims=True) + epsilon)
                n2_ref[at, :] = (values * scale * gain_ref[1:2, :]).astype(jnp.bfloat16)
                return carry

            lax.fori_loop(0, own // 32, middle, 0)
        kind = step - 1
        for step_from in (1, 3, 2):
            for copy in f_z_in(kind, step_from):
                copy.wait_recv()
            f_x(kind, step_from).start()
            f_c(kind, step_from, 0).start()
        d_z_in(step).wait_recv()
        if step < z_size - 1:
            d_z(step).start()
        d_y(step).start()
    for kind in range(3):
        for step in (0, 1, 3, 2):
            f_x_in(kind, step).wait_recv()
            f_c(kind, step, 1).start()
    for kind in range(3):
        for step in range(z_size):
            for far in range(2):
                f_c_in(kind, step, far).wait_recv()
    for step in range(z_size):
        d_y_in(step).wait_recv()

    kv_y.wait_send()
    tok_y.wait_send()
    part_out.wait_send()
    own_d.wait()
    for copy in saves:
        copy.wait()
    for step in range(z_size):
        d_y(step).wait_send()
        if step < z_size - 1:
            d_z(step).wait_send()
        for kind in range(3):
            if step < z_size - 1:
                a_z(kind, step).wait_send()
            if step:
                for copy in f_z(kind, step):
                    copy.wait_send()
            a_x(kind, step).wait_send()
            f_x(kind, step).wait_send()
            for far in range(2):
                a_c(kind, step, far).wait_send()
                f_c(kind, step, far).wait_send()


def pre_call(tokens, kv_gains, table, allowed, cotangent, w_query, w_out, ffn):
    z_size = lax.axis_size("z")
    own, width = tokens.shape
    seq = 2 * own
    rows, cols = w_query.shape
    head = table.shape[2] * 2
    units = ragged_split(ffn[0].shape[1], z_size)[1]
    low = lambda *dims: jax.ShapeDtypeStruct(dims, jnp.bfloat16)
    full = lambda *dims: jax.ShapeDtypeStruct(dims, jnp.float32)
    dma = lambda *lead: pltpu.SemaphoreType.DMA(lead)
    vmem = pl.BlockSpec(memory_space=pltpu.VMEM)
    hbm = pl.BlockSpec(memory_space=pl.ANY)
    wide = lambda *lead: pltpu.VMEM((*lead, width), jnp.bfloat16)
    return pl.pallas_call(
        functools.partial(pre_kernel, z_size),
        out_shape=(
            low(seq, width),
            low(seq, cols),
            low(seq, head),
            low(seq, head),
            low(seq, cols),
            full(own, width),
            low(own, width),
            full(8, width),
            low(width, kv_gains.shape[1]),
            low(width, cols),
            low(width, cols),
            low(3, width, units),
            low(z_size, seq, width),
        ),
        in_specs=[vmem] * 4 + [hbm] * 6,
        out_specs=(vmem,) * 8 + (hbm,) * 5,
        scratch_shapes=[
            pltpu.VMEM((width, kv_gains.shape[1]), jnp.bfloat16),
            pltpu.VMEM((width, cols), jnp.bfloat16),
            pltpu.VMEM((width, cols), jnp.bfloat16),
            wide(seq),
            wide(seq),
            wide(own),
            dma(3),
            dma(3),
            dma(3, z_size),
            dma(3, z_size),
            dma(3, z_size),
            dma(3, z_size),
            dma(3, 2 * z_size),
            dma(3, 2 * z_size),
            dma(3, z_size, 2),
            dma(3, z_size, 2),
            dma(3, z_size),
            dma(3, z_size),
            dma(3, 2 * z_size),
            dma(3, 2 * z_size),
            dma(z_size),
            dma(z_size),
            dma(z_size),
            dma(z_size),
            dma(16),
        ],
        compiler_params=pltpu.CompilerParams(
            collective_id=1, has_side_effects=True, vmem_limit_bytes=VMEM_BYTES
        ),
        cost_estimate=pl.CostEstimate(
            flops=8 * seq * width * cols,
            bytes_accessed=8 * width * (cols + units),
            transcendentals=seq * seq * cols // head,
        ),
    )(tokens, kv_gains, table, allowed, cotangent, w_query, w_out, *ffn)


def norm_back(values, gain, upstream):
    scale = lax.rsqrt(jnp.mean(values * values, axis=-1, keepdims=True) + epsilon)
    normed = values * scale
    pulled = gain * upstream
    back = scale * (pulled - normed * jnp.mean(normed * pulled, axis=-1, keepdims=True))
    return back, jnp.sum(upstream * normed, axis=0, keepdims=True)


def post_kernel(
    z_size,
    main,
    gn_ref,
    mid_ref,
    tok_ref,
    cot_ref,
    gain_ref,
    n1_ref,
    rot_ref,
    key_ref,
    val_ref,
    att_ref,
    table_ref,
    allow_ref,
    kv_hbm,
    wq_hbm,
    wo_hbm,
    mix_hbm,
    ffn_hbm,
    mixed_ref,
    tgrad_ref,
    gsum_ref,
    kvg_ref,
    qg_ref,
    og_ref,
    wg_out,
    wu_out,
    wd_out,
    kv_w,
    q_w,
    o_w,
    o_part,
    gm,
    gm_f,
    gq,
    gkv,
    kv_sum,
    back_y,
    mix_y,
    mix_z,
    mix_s,
    o_c,
    o_x,
    o_z,
    q_c,
    q_x,
    q_z,
    kv_y,
    kv_c,
    kv_x,
    kv_z,
    gain_own,
    gain_in,
    ffn_in,
    ffn_sum,
    load_sem,
    ffn_sem,
    y_send,
    y_recv,
    my_send,
    my_recv,
    mz_send,
    mz_recv,
    wc_send,
    wc_recv,
    wx_send,
    wx_recv,
    wz_send,
    wz_recv,
    kc_send,
    kc_recv,
    kz_send,
    kz_recv,
    g_send,
    g_recv,
):
    me_z, me_x = lax.axis_index("z"), lax.axis_index("x")
    me_c, me_y = lax.axis_index("c"), lax.axis_index("mp")
    own, width = tok_ref.shape
    seq = 2 * own
    head = key_ref.shape[1]
    cols_here = att_ref.shape[1]
    heads = cols_here // head
    rows = qg_ref.shape[0]
    span = width // z_size
    mine = pl.ds(pl.multiple_of(me_y * own, own), own)
    theirs = pl.ds(pl.multiple_of((1 - me_y) * own, own), own)
    to_y, to_x, to_c = {"mp": 1 - me_y}, {"x": 1 - me_x}, {"c": 1 - me_c}
    head_scale = head ** (-0.5)

    def behind(step):
        return lax.rem(me_z - step + z_size, z_size)

    def to_z(step):
        return {"z": lax.rem(me_z + step, z_size)}

    def row_block(step, x_at, c_at):
        start = ((behind(step) * 2 + x_at) * 2 + c_at) * rows
        return pl.ds(pl.multiple_of(start, rows), rows)

    loads = [
        pltpu.make_async_copy(wo_hbm, o_w, load_sem.at[0]),
        pltpu.make_async_copy(wq_hbm, q_w, load_sem.at[1]),
        pltpu.make_async_copy(
            kv_hbm.at[:, :, :, :, :, pl.ds(0, 2 * head)], kv_w, load_sem.at[2]
        ),
    ]
    for step in range(z_size):
        loads.append(
            pltpu.make_async_copy(mix_hbm.at[step, mine], mix_s.at[step], load_sem.at[3 + step])
        )
    for load in loads:
        load.start()

    barrier = pltpu.get_barrier_semaphore()
    peers = [to_y, to_x, to_c] + [to_z(step) for step in range(1, z_size)]
    for where in peers:
        pl.semaphore_signal(barrier, inc=1, device_id=where, device_id_type=MESH_ID)
    pl.semaphore_wait(barrier, len(peers))

    def mid_rows(index, total):
        at = pl.ds(pl.multiple_of(index * 32, 32), 32)
        grad, gain_part = norm_back(mid_ref[at, :], gain_ref[1:2, :], gn_ref[at, :])
        grad = grad + cot_ref[at, :].astype(jnp.float32)
        gm_f[at, :] = grad
        gm[pl.ds(pl.multiple_of(me_y * own + index * 32, 32), 32), :] = grad.astype(jnp.bfloat16)
        return total + gain_part

    ffn_gain_part = lax.fori_loop(
        0, own // 32, mid_rows, jnp.zeros((1, width), jnp.float32)
    )
    gm_y = remote(gm.at[mine], gm.at[mine], y_send.at[0], y_recv.at[0], to_y)
    gm_y_in = remote(gm.at[theirs], gm.at[theirs], y_send.at[0], y_recv.at[0], to_y)
    gm_y.start()

    def mix_over_y(step):
        return remote(
            mix_hbm.at[step, theirs], mix_y.at[step], my_send.at[step], my_recv.at[step], to_y
        )

    def mix_over_z(step):
        return remote(
            mix_s.at[step], mix_z.at[step - 1], mz_send.at[step], mz_recv.at[step - 1], to_z(1)
        )

    def mix_step(step):
        mix_over_y(step).wait_recv()
        slot = (step - 2) % z_size
        others = [mix_y.at[step]]
        if step != 1:
            remote(
                mix_s.at[1], mix_z.at[slot], mz_send.at[1], mz_recv.at[slot], to_z(1)
            ).wait_recv()
            others.append(mix_z.at[slot])
        if step:
            add_rows(mix_s.at[step], others, mix_s.at[step], own)
            mix_over_z(step).start()
        else:
            add_rows(mid_ref, [mix_s.at[0], *others], mixed_ref, own)

    for step in (1, 2, 3, 0):
        mix_over_y(step).start()

    outs = (wg_out, wu_out, wd_out)
    half = rows // 2

    def ffn_load(index):
        at = pl.ds(index % 2 * half, half)
        return pltpu.make_async_copy(ffn_hbm.at[index // 2, :, at], ffn_in, ffn_sem.at[0])

    def ffn_save(index):
        at = pl.ds(index % 2 * half, half)
        return pltpu.make_async_copy(ffn_sum, outs[index // 2].at[at], ffn_sem.at[1])

    ffn_load(0).start()

    def place(index):
        ffn_load(index).wait()
        if index:
            ffn_save(index - 1).wait()
        ffn_sum[:, z_size * main :] = jnp.zeros((half, 128 * z_size // 2), jnp.float32)
        for step in range(z_size):
            at = behind(step)
            body = pl.ds(pl.multiple_of(at * main, 128), main)
            ffn_sum[:, body] = ffn_in[step, :, :main].astype(jnp.float32)
            tail = pl.ds(pl.multiple_of(z_size * main + at // 2 * 128, 128), 128)
            ffn_sum[:, tail] += ffn_in[step, :, main:].astype(jnp.float32)
        ffn_save(index).start()
        if index < 5:
            ffn_load(index + 1).start()

    kinds = ((o_part, o_c, o_x, o_z, og_ref), (o_w, q_c, q_x, q_z, qg_ref))

    def w_c(kind, step, far):
        x_at = 1 - me_x if far else me_x
        return remote(
            kinds[kind][0].at[row_block(step, x_at, 1 - me_c)],
            kinds[kind][1].at[step, far],
            wc_send.at[kind, step, far],
            wc_recv.at[kind, step, far],
            to_c,
        )

    def w_x(kind, step):
        return remote(
            kinds[kind][0].at[row_block(step, 1 - me_x, me_c)],
            kinds[kind][2].at[step],
            wx_send.at[kind, step],
            wx_recv.at[kind, step],
            to_x,
        )

    def w_z(kind, step):
        return remote(
            kinds[kind][0].at[row_block(step, me_x, me_c)],
            kinds[kind][3].at[step - 1],
            wz_send.at[kind, step],
            wz_recv.at[kind, step - 1],
            to_z(1),
        )

    def w_x_stage(kind, step):
        w_c(kind, step, 1).wait_recv()
        block = kinds[kind][0].at[row_block(step, 1 - me_x, me_c)]
        add_rows(block, [kinds[kind][1].at[step, 1]], block, rows)
        w_x(kind, step).start()

    def w_z_stage(kind, step):
        part, from_c, from_x, from_z, result = kinds[kind]
        w_c(kind, step, 0).wait_recv()
        w_x(kind, step).wait_recv()
        others = [from_c.at[step, 0], from_x.at[step]]
        slot = (step - 2) % z_size
        if step != 1:
            remote(
                from_z.at[slot],
                from_z.at[slot],
                wz_send.at[kind, 1],
                wz_recv.at[kind, slot],
                to_z(1),
            ).wait_recv()
            others.append(from_z.at[slot])
        block = part.at[row_block(step, me_x, me_c)]
        if step:
            add_rows(block, others, block, rows)
            w_z(kind, step).start()
        else:
            add_rows(block, others, result, rows)

    def w_product(kind, step, left, right):
        at = pl.ds(pl.multiple_of(behind(step) * span, 128), span)
        turned = left[:, at].T

        def tile_body(tile, carry):
            cols = pl.ds(pl.multiple_of(tile * TILE, TILE), TILE)
            kinds[kind][0][at, cols] = dot_nn(turned, right[:, cols]).astype(jnp.bfloat16)
            return carry

        lax.fori_loop(0, cols_here // TILE, tile_body, 0)
        for far in (1, 0):
            w_c(kind, step, far).start()

    order = (1, 2, 3, 0)
    gm_y_in.wait_recv()
    w_product(0, 1, gm, att_ref)
    w_product(0, 2, gm, att_ref)
    w_x_stage(0, 1)
    w_product(0, 3, gm, att_ref)
    w_x_stage(0, 2)
    w_product(0, 0, gm, att_ref)
    w_x_stage(0, 3)
    for load in loads:
        load.wait()

    kv_sum[...] = jnp.zeros(kv_sum.shape, jnp.float32)
    table = (table_ref[0], table_ref[1])

    def attend_back(index, carry):
        cols = pl.ds(pl.multiple_of(index * head, head), head)
        grad_vals = dot_nn(gm[...], o_w[:, cols]).astype(jnp.bfloat16)
        rotated = rot_ref[:, cols]
        probs = head_probs(rotated, key_ref[...], allow_ref[...])
        grad_probs = matmul_nt(grad_vals, val_ref[...])
        delta = jnp.sum(probs * grad_probs, axis=-1, keepdims=True)
        grad_scores = (probs * (grad_probs - delta)).astype(jnp.bfloat16)
        grad_rot = dot_nn(grad_scores, key_ref[...])
        gq[:, cols] = (spin_back(grad_rot, table) * head_scale).astype(jnp.bfloat16)
        kv_sum[0] += matmul_tn(grad_scores, rotated)
        kv_sum[1] += matmul_tn(probs.astype(jnp.bfloat16), grad_vals)
        return carry

    lax.fori_loop(0, heads, attend_back, 0)
    w_x_stage(0, 0)
    gkv[:, :head] = spin_back(kv_sum[0], table).astype(jnp.bfloat16)
    gkv[:, head:] = kv_sum[1].astype(jnp.bfloat16)

    w_product(1, 1, n1_ref, gq)
    mix_step(1)
    w_product(1, 2, n1_ref, gq)
    w_x_stage(1, 1)
    w_z_stage(0, 1)
    w_product(1, 3, n1_ref, gq)
    w_x_stage(1, 2)
    w_product(1, 0, n1_ref, gq)
    w_x_stage(1, 3)
    w_x_stage(1, 0)
    mix_step(2)

    gm_y.wait_send()
    back = gm
    def input_tile(index, carry):
        at = pl.ds(pl.multiple_of(index * span, 128), span)
        back[:, at] = (
            matmul_nt(gq[...], q_w[at, :]) + matmul_nt(gkv[...], kv_w[index].reshape(span, 2 * head))
        ).astype(jnp.bfloat16)
        return carry

    lax.fori_loop(0, z_size, input_tile, 0)
    back_out = remote(back.at[theirs], back_y, y_send.at[1], y_recv.at[1], to_y)
    back_out.start()

    kv_part = kv_w

    def kv_tile(index, carry):
        at = pl.ds(pl.multiple_of(index * span, 128), span)
        product = dot_nn(n1_ref[:, at].T, gkv[...]).astype(jnp.bfloat16)
        kv_part[index] = product.reshape(kv_part.shape[1:])
        return carry

    lax.fori_loop(0, z_size, kv_tile, 0)
    kv_over_y = remote(kv_part.at[:, :, :, 1 - me_y], kv_y, y_send.at[2], y_recv.at[2], to_y)
    kv_over_y.start()
    w_z_stage(0, 2)
    mix_step(3)
    place(0)
    place(1)
    kv_over_y.wait_recv()

    def kv_add_y(index, carry):
        for x_at in range(2):
            for c_at in range(2):
                block = kv_part.at[index, x_at, c_at, me_y]
                block[...] = (
                    block[...].astype(jnp.float32) + kv_y[index, x_at, c_at].astype(jnp.float32)
                ).astype(jnp.bfloat16)
        return carry

    lax.fori_loop(0, z_size, kv_add_y, 0)
    kv_over_c = remote(
        kv_part.at[:, :, 1 - me_c, me_y], kv_c, kc_send.at[0], kc_recv.at[0], to_c
    )
    kv_over_c.start()
    w_z_stage(0, 3)
    w_z_stage(1, 1)
    kv_over_c.wait_recv()

    def kv_add_c(index, carry):
        for x_at in range(2):
            block = kv_part.at[index, x_at, me_c, me_y]
            block[...] = (
                block[...].astype(jnp.float32) + kv_c[index, x_at].astype(jnp.float32)
            ).astype(jnp.bfloat16)
        return carry

    lax.fori_loop(0, z_size, kv_add_c, 0)
    kv_over_x = remote(
        kv_part.at[:, 1 - me_x, me_c, me_y], kv_x, kc_send.at[1], kc_recv.at[1], to_x
    )
    kv_over_x.start()

    back_out.wait_recv()

    def input_rows(index, total):
        at = pl.ds(pl.multiple_of(index * 32, 32), 32)
        there = pl.ds(pl.multiple_of(me_y * own + index * 32, 32), 32)
        upstream = back[there, :].astype(jnp.float32) + back_y[at, :].astype(jnp.float32)
        grad, gain_part = norm_back(
            tok_ref[at, :].astype(jnp.float32), gain_ref[0:1, :], upstream
        )
        tgrad_ref[at, :] = (gm_f[at, :] + grad).astype(jnp.bfloat16)
        return total + gain_part

    attn_gain_part = lax.fori_loop(
        0, own // 32, input_rows, jnp.zeros((1, width), jnp.float32)
    )
    gain_own[0, 0:1, :] = attn_gain_part
    gain_own[0, 1:2, :] = ffn_gain_part
    gain_own[0, 2:8, :] = jnp.zeros((6, width), jnp.float32)

    def gain_send(stage, where):
        return remote(
            gain_own.at[stage], gain_in.at[stage], g_send.at[stage], g_recv.at[stage], where
        )

    gain_hops = [gain_send(0, to_y), gain_send(1, to_c), gain_send(2, to_x)]
    gain_last = [
        remote(
            gain_own.at[3], gain_in.at[2 + step], g_send.at[2 + step], g_recv.at[2 + step], to_z(step)
        )
        for step in range(1, z_size)
    ]

    def gain_fold(stage):
        gain_hops[stage].wait_recv()
        gain_own[stage + 1] = gain_own[stage] + gain_in[stage]

    gain_hops[0].start()
    mix_step(0)
    w_z_stage(0, 0)
    gain_fold(0)
    gain_hops[1].start()
    w_z_stage(1, 2)
    gain_fold(1)
    gain_hops[2].start()
    place(2)
    place(3)
    gain_fold(2)
    for copy in gain_last:
        copy.start()

    kv_over_x.wait_recv()

    def kv_add_x(index, carry):
        block = kv_part.at[index, me_x, me_c, me_y]
        block[...] = (
            block[...].astype(jnp.float32) + kv_x[index].astype(jnp.float32)
        ).astype(jnp.bfloat16)
        return carry

    lax.fori_loop(0, z_size, kv_add_x, 0)
    kv_over_z = [
        remote(
            kv_part.at[lax.rem(me_z + step, z_size), me_x, me_c, me_y],
            kv_z.at[step],
            kz_send.at[step],
            kz_recv.at[step],
            to_z(step),
        )
        for step in range(1, z_size)
    ]
    for copy in kv_over_z:
        copy.start()
    w_z_stage(1, 3)
    place(4)
    place(5)
    for copy in gain_last:
        copy.wait_recv()
    gsum_ref[...] = gain_own[3] + gain_in[3] + gain_in[4] + gain_in[5]
    for copy in kv_over_z:
        copy.wait_recv()
    kvg_ref[...] = (
        kv_part[me_z, me_x, me_c, me_y].astype(jnp.float32)
        + kv_z[1].astype(jnp.float32)
        + kv_z[2].astype(jnp.float32)
        + kv_z[3].astype(jnp.float32)
    )
    w_z_stage(1, 0)

    back_out.wait_send()
    kv_over_y.wait_send()
    kv_over_c.wait_send()
    kv_over_x.wait_send()
    ffn_save(5).wait()
    for copy in gain_hops + gain_last + kv_over_z:
        copy.wait_send()
    for step in range(z_size):
        mix_over_y(step).wait_send()
        if step:
            mix_over_z(step).wait_send()
        for kind in range(2):
            w_c(kind, step, 0).wait_send()
            w_c(kind, step, 1).wait_send()
            w_x(kind, step).wait_send()
            if step:
                w_z(kind, step).wait_send()


def post_call(
    grad_normed,
    mid,
    tokens,
    cotangent,
    gains,
    normed_one,
    rotated,
    keys,
    values,
    attn_vals,
    table,
    allowed,
    kv_weight,
    query_weight,
    out_weight,
    mix_parts,
    ffn_grads,
    ffn_cols,
):
    z_size = lax.axis_size("z")
    own, width = tokens.shape
    seq = 2 * own
    head = keys.shape[1]
    cols = attn_vals.shape[1]
    rows = width // (4 * z_size)
    main, units = ragged_split(ffn_cols, z_size)
    low = lambda *dims: pltpu.VMEM(dims, jnp.bfloat16)
    full = lambda *dims: pltpu.VMEM(dims, jnp.float32)
    out_full = lambda *dims: jax.ShapeDtypeStruct(dims, jnp.float32)
    out_low = lambda *dims: jax.ShapeDtypeStruct(dims, jnp.bfloat16)
    dma = lambda *lead: pltpu.SemaphoreType.DMA(lead)
    vmem = pl.BlockSpec(memory_space=pltpu.VMEM)
    hbm = pl.BlockSpec(memory_space=pl.ANY)
    z = z_size
    return pl.pallas_call(
        functools.partial(post_kernel, z_size, main),
        out_shape=(
            out_low(own, width),
            out_low(own, width),
            out_full(8, width),
            out_full(rows // 2, 2 * head),
            out_full(rows, cols),
            out_full(rows, cols),
            out_full(rows, ffn_cols),
            out_full(rows, ffn_cols),
            out_full(rows, ffn_cols),
        ),
        in_specs=[vmem] * 12 + [hbm] * 5,
        out_specs=(vmem,) * 6 + (hbm,) * 3,
        scratch_shapes=[
            low(z, 2, 2, 2, rows // 2, 2 * head),
            low(width, cols),
            low(width, cols),
            low(width, cols),
            low(seq, width),
            full(own, width),
            low(seq, cols),
            low(seq, 2 * head),
            full(2, seq, head),
            low(own, width),
            low(z, own, width),
            low(z - 1, own, width),
            low(z, own, width),
            low(z, 2, rows, cols),
            low(z, rows, cols),
            low(z - 1, rows, cols),
            low(z, 2, rows, cols),
            low(z, rows, cols),
            low(z - 1, rows, cols),
            low(z, 2, 2, rows // 2, 2 * head),
            low(z, 2, rows // 2, 2 * head),
            low(z, rows // 2, 2 * head),
            low(z, rows // 2, 2 * head),
            full(4, 8, width),
            full(6, 8, width),
            low(z, rows // 2, units),
            full(rows // 2, ffn_cols),
            dma(3 + z),
            dma(2),
            dma(3),
            dma(3),
            dma(z),
            dma(z),
            dma(z),
            dma(z),
            dma(2, z, 2),
            dma(2, z, 2),
            dma(2, z),
            dma(2, z),
            dma(2, z),
            dma(2, z),
            dma(2),
            dma(2),
            dma(z),
            dma(z),
            dma(6),
            dma(6),
        ],
        compiler_params=pltpu.CompilerParams(
            collective_id=2, has_side_effects=True, vmem_limit_bytes=VMEM_BYTES
        ),
        cost_estimate=pl.CostEstimate(
            flops=14 * seq * width * cols,
            bytes_accessed=10 * width * cols,
            transcendentals=seq * seq * cols // head,
        ),
    )(
        grad_normed,
        mid,
        tokens,
        cotangent,
        gains,
        normed_one,
        rotated,
        keys,
        values,
        attn_vals,
        table,
        allowed,
        kv_weight.reshape(z, 2, 2, 2, rows // 2, kv_weight.shape[1]),
        query_weight,
        out_weight,
        mix_parts,
        ffn_grads,
    )


FF_SPLIT = 4


def ffn_pass(normed, grad_out, gate_weight, up_weight, down_weight):
    gate = jnp.dot(normed, gate_weight, preferred_element_type=jnp.float32)
    up_proj = jnp.dot(normed, up_weight, preferred_element_type=jnp.float32)
    grad_hidden = jnp.dot(grad_out, down_weight, preferred_element_type=jnp.float32)
    product, pull = jax.vjp(gelu_product, gate, up_proj)
    hidden = product.astype(jnp.bfloat16)
    grad_gate_f, grad_up_f = pull(grad_hidden)
    grad_gate = grad_gate_f.astype(jnp.bfloat16)
    grad_up = grad_up_f.astype(jnp.bfloat16)
    mixed_part = matmul_nt(hidden, down_weight).astype(jnp.bfloat16)
    normed_part = (matmul_nt(grad_gate, gate_weight) + matmul_nt(grad_up, up_weight)).astype(
        jnp.bfloat16
    )
    weight_parts = [
        matmul_tn(normed, grad_gate).astype(jnp.bfloat16),
        matmul_tn(normed, grad_up).astype(jnp.bfloat16),
        matmul_tn(grad_out, hidden).astype(jnp.bfloat16),
    ]
    return mixed_part, normed_part, weight_parts


def shards_general(
    tokens,
    segments,
    positions,
    cotangent,
    attn_gain,
    ffn_gain,
    w_kv,
    w_query,
    w_out,
    w_gate,
    w_up,
    w_down,
):
    everywhere = ("z", "xc", "mp")
    dp = ("z", "xc")
    z_size = lax.axis_size("z")
    xc_size = lax.axis_size("xc")
    gains = lax.all_gather(
        jnp.stack([attn_gain, ffn_gain], axis=1), everywhere, axis=0, tiled=True
    ).astype(jnp.float32)
    gain_one, gain_two = gains[:, 0], gains[:, 1]
    kv_weight = lax.all_gather(w_kv, everywhere, axis=0, tiled=True)
    head_dim = kv_weight.shape[1] // 2
    width = tokens.shape[1]
    seq_len = segments.shape[0]
    heads_here = w_query.shape[1] // head_dim
    scale = head_dim ** (-0.5)
    cosine, sine = rotary_angles(positions, head_dim)
    inputs_f = tokens.astype(jnp.float32)
    tokens_all = lax.all_gather(tokens, "mp", axis=0, tiled=True)
    normed_one = norm_gain(tokens_all.astype(jnp.float32), gain_one).astype(jnp.bfloat16)
    query_weight = lax.all_gather(w_query, dp, axis=0, tiled=True)
    out_weight = lax.all_gather(w_out, dp, axis=0, tiled=True)

    rows = w_gate.shape[0]
    unit = w_gate.shape[1] // z_size

    def spread(weight):
        pieces = weight.reshape(rows, z_size, unit).transpose(1, 0, 2)
        pieces = lax.all_to_all(pieces, "z", split_axis=0, concat_axis=0, tiled=True)
        return lax.all_gather(pieces, "xc", axis=1, tiled=False).reshape(width, unit)

    gate_weight, up_weight, down_weight = spread(w_gate), spread(w_up), spread(w_down)
    grad_all = lax.all_gather(cotangent, ("z", "mp"), axis=0, tiled=True)

    query = jnp.dot(normed_one, query_weight, preferred_element_type=jnp.float32).reshape(
        seq_len, heads_here, head_dim
    )
    rotated = (rotate(query, cosine[:, None], sine[:, None]) * scale).astype(jnp.bfloat16)
    keyval = jnp.dot(normed_one, kv_weight, preferred_element_type=jnp.float32)
    keys = rotate(keyval[:, :head_dim], cosine, sine).astype(jnp.bfloat16)
    values = keyval[:, head_dim:].astype(jnp.bfloat16)
    allowed = block_allowed(segments, 0, seq_len)
    scores = jnp.einsum("thd,sd->hts", rotated, keys, preferred_element_type=jnp.float32)
    scores = jnp.where(allowed[None], scores, masked_score)
    row_max = jnp.max(scores, axis=-1, keepdims=True)
    weights = jnp.exp(scores - row_max)
    probs = weights / jnp.sum(weights, axis=-1, keepdims=True)
    probs_low = probs.astype(jnp.bfloat16)
    attn_vals = (
        jnp.einsum("hts,sd->thd", probs_low, values, preferred_element_type=jnp.float32)
        .reshape(seq_len, heads_here * head_dim)
        .astype(jnp.bfloat16)
    )
    mid = inputs_f + lax.psum_scatter(
        matmul_nt(attn_vals, out_weight).astype(jnp.bfloat16),
        "mp",
        scatter_dimension=0,
        tiled=True,
    ).astype(jnp.float32)
    normed_two = norm_gain(mid, gain_two).astype(jnp.bfloat16)
    normed_all = lax.all_gather(normed_two, ("z", "mp"), axis=0, tiled=True)

    mixed_part, normed_part, weight_parts = ffn_pass(
        normed_all, grad_all, gate_weight, up_weight, down_weight
    )
    grad_normed_two = lax.psum_scatter(
        normed_part, ("z", "mp"), scatter_dimension=0, tiled=True
    ).astype(jnp.float32)
    mixed = (
        mid
        + lax.psum_scatter(mixed_part, ("z", "mp"), scatter_dimension=0, tiled=True).astype(
            jnp.float32
        )
    ).astype(jnp.bfloat16)

    def collect(part):
        pieces = part.reshape(z_size, xc_size, rows, unit).transpose(1, 0, 2, 3)
        pieces = pieces.reshape(xc_size * z_size * rows, unit)
        pieces = lax.psum_scatter(pieces, "xc", scatter_dimension=0, tiled=True)
        pieces = pieces.reshape(z_size, rows, unit)
        pieces = lax.all_to_all(pieces, "z", split_axis=0, concat_axis=0, tiled=True)
        return pieces.transpose(1, 0, 2).reshape(rows, z_size * unit).astype(jnp.float32)

    w_gate_grad, w_up_grad, w_down_grad = [collect(part) for part in weight_parts]

    norm_pull_two = jax.vjp(norm_gain, mid, gain_two)[1]
    grad_mid_norm, grad_gain_two = norm_pull_two(grad_normed_two)
    grad_mid = cotangent.astype(jnp.float32) + grad_mid_norm
    grad_mid_all = lax.all_gather(grad_mid.astype(jnp.bfloat16), "mp", axis=0, tiled=True)
    grad_vals = (
        jnp.dot(grad_mid_all, out_weight, preferred_element_type=jnp.float32)
        .astype(jnp.bfloat16)
        .reshape(seq_len, heads_here, head_dim)
    )
    grad_probs = jnp.einsum("thd,sd->hts", grad_vals, values, preferred_element_type=jnp.float32)
    delta = jnp.sum(probs * grad_probs, axis=-1, keepdims=True)
    grad_scores = (probs * (grad_probs - delta)).astype(jnp.bfloat16)
    grad_rot = jnp.einsum("hts,sd->thd", grad_scores, keys, preferred_element_type=jnp.float32)
    key_sum = jnp.einsum("hts,thd->sd", grad_scores, rotated, preferred_element_type=jnp.float32)
    value_sum = jnp.einsum("hts,thd->sd", probs_low, grad_vals, preferred_element_type=jnp.float32)
    grad_query = (
        (unrotate(grad_rot, cosine[:, None], sine[:, None]) * scale)
        .reshape(seq_len, heads_here * head_dim)
        .astype(jnp.bfloat16)
    )
    grad_kv = jnp.concatenate([unrotate(key_sum, cosine, sine), value_sum], axis=1).astype(
        jnp.bfloat16
    )
    grad_normed_one = lax.psum_scatter(
        (matmul_nt(grad_query, query_weight) + matmul_nt(grad_kv, kv_weight)).astype(jnp.bfloat16),
        "mp",
        scatter_dimension=0,
        tiled=True,
    ).astype(jnp.float32)
    norm_pull_one = jax.vjp(norm_gain, inputs_f, gain_one)[1]
    grad_input_norm, grad_gain_one = norm_pull_one(grad_normed_one)
    tokens_grad = (grad_mid + grad_input_norm).astype(jnp.bfloat16)

    w_query_grad = lax.psum_scatter(
        matmul_tn(normed_one, grad_query).astype(jnp.bfloat16), dp, scatter_dimension=0, tiled=True
    ).astype(jnp.float32)
    w_out_grad = lax.psum_scatter(
        matmul_tn(grad_mid_all, attn_vals).astype(jnp.bfloat16), dp, scatter_dimension=0, tiled=True
    ).astype(jnp.float32)
    small = jnp.concatenate(
        [matmul_tn(normed_one, grad_kv), grad_gain_one[:, None], grad_gain_two[:, None]], axis=1
    )
    small = lax.psum_scatter(small, everywhere, scatter_dimension=0, tiled=True)
    kv_grad = small[:, : 2 * head_dim]
    return (
        mixed,
        tokens_grad,
        small[:, 2 * head_dim],
        small[:, 2 * head_dim + 1],
        kv_grad,
        w_query_grad,
        w_out_grad,
        w_gate_grad,
        w_up_grad,
        w_down_grad,
    )


def shards_fast(
    tokens,
    segments,
    positions,
    cotangent,
    attn_gain,
    ffn_gain,
    w_kv,
    w_query,
    w_out,
    w_gate,
    w_up,
    w_down,
):
    seq_len = segments.shape[0]
    cosine, sine = rotary_angles(positions, w_kv.shape[1] // 2)
    table = jnp.stack(
        [
            jnp.concatenate([cosine, cosine], axis=1),
            jnp.concatenate([-sine, sine], axis=1),
        ]
    )
    allowed = block_allowed(segments, 0, seq_len).astype(jnp.float32)
    kv_gains = jnp.concatenate(
        [w_kv, attn_gain[:, None], ffn_gain[:, None], jnp.zeros((w_kv.shape[0], 126), w_kv.dtype)],
        axis=1,
    )
    (
        normed_one,
        rotated,
        keys,
        values,
        attn_vals,
        mid,
        normed_two,
        gains,
        kv_weight,
        query_weight,
        out_weight,
        ffn_weights,
        grad_all,
    ) = pre_call(
        tokens, kv_gains, table, allowed, cotangent, w_query, w_out, (w_gate, w_up, w_down)
    )
    main = ragged_split(w_gate.shape[1], lax.axis_size("z"))[0]
    grad_normed_two, mix_parts, ffn_grads = ffn_call(
        normed_two, grad_all, ffn_weights, w_gate.shape[0], main
    )
    mixed, tokens_grad, gain_grads, kv_grad, query_grad, out_grad, *ffn_out = post_call(
        grad_normed_two,
        mid,
        tokens,
        cotangent,
        gains,
        normed_one,
        rotated,
        keys,
        values,
        attn_vals,
        table,
        allowed,
        kv_weight,
        query_weight,
        out_weight,
        mix_parts,
        ffn_grads,
        w_gate.shape[1],
    )
    share = attn_gain.shape[0]
    place = lax.axis_index(("z", "x", "c", "mp")) * share
    gain_grads = lax.dynamic_slice(gain_grads, (0, place), (2, share))
    return (
        mixed,
        tokens_grad,
        gain_grads[0],
        gain_grads[1],
        kv_grad,
        query_grad,
        out_grad,
        *ffn_out,
    )


def solution(mesh):
    dp_size, mp_size = mesh.shape["dp"], mesh.shape["mp"]
    if dp_size == 4 * FF_SPLIT and mp_size == 2:
        body, dp = shards_fast, ("z", "x", "c")
        sizes = (FF_SPLIT, 2, 2, mp_size)
    else:
        body, dp = shards_general, ("z", "xc")
        sizes = (FF_SPLIT, dp_size // FF_SPLIT, mp_size)
    all_axes = (*dp, "mp")
    fine = jax.sharding.Mesh(mesh.devices.reshape(sizes), all_axes)
    in_specs = (
        P(all_axes, None),
        P(dp),
        P(dp),
        P(all_axes, None),
        P(all_axes),
        P(all_axes),
        P(all_axes, None),
        P(dp, "mp"),
        P(dp, "mp"),
        P(dp, "mp"),
        P(dp, "mp"),
        P(dp, "mp"),
    )
    out_specs = (
        P(all_axes, None),
        P(all_axes, None),
        P(all_axes),
        P(all_axes),
        P(all_axes, None),
        P(dp, "mp"),
        P(dp, "mp"),
        P(dp, "mp"),
        P(dp, "mp"),
        P(dp, "mp"),
    )
    return jax.shard_map(body, mesh=fine, in_specs=in_specs, out_specs=out_specs, check_vma=False)
```

```python
import functools

import jax
import jax.numpy as jnp
from jax import lax
from jax.experimental import pallas as pl
from jax.experimental.pallas import tpu as pltpu
from jax.sharding import PartitionSpec as P

WINDOW = 2048


epsilon = 1e-06
rope_base = 10000.0
masked_score = -1e30
VMEM_BYTES = 66_000_000


def norm_gain(values, gain):
    return values * lax.rsqrt(jnp.mean(values * values, axis=-1, keepdims=True) + epsilon) * gain


def rotary_angles(positions, head_width):
    quarter = head_width // 4
    freqs = rope_base ** (-jnp.arange(quarter).astype(jnp.float32) / quarter)
    phase = positions.astype(jnp.float32)[:, None] * freqs[None, :]
    return (jnp.cos(phase), jnp.sin(phase))


def rotate(values, cosine, sine):
    quarter = cosine.shape[-1]
    first_half = values[..., :quarter]
    second_half = values[..., quarter : 2 * quarter]
    return jnp.concatenate(
        [
            first_half * cosine - second_half * sine,
            second_half * cosine + first_half * sine,
            values[..., 2 * quarter :],
        ],
        axis=-1,
    )


def unrotate(values, cosine, sine):
    quarter = cosine.shape[-1]
    first_half = values[..., :quarter]
    second_half = values[..., quarter : 2 * quarter]
    return jnp.concatenate(
        [
            first_half * cosine + second_half * sine,
            second_half * cosine - first_half * sine,
            values[..., 2 * quarter :],
        ],
        axis=-1,
    )


def gelu_product(gate, up_proj):
    return jax.nn.gelu(gate, approximate=True) * up_proj


def matmul_nt(left, right):
    return lax.dot_general(
        left, right, (((1,), (1,)), ((), ())), preferred_element_type=jnp.float32
    )


def matmul_tn(left, right):
    return lax.dot_general(
        left, right, (((0,), (0,)), ((), ())), preferred_element_type=jnp.float32
    )


def block_allowed(segments, first_row, rows):
    seq_len = segments.shape[0]
    query_rows = first_row + jnp.arange(rows)
    key_rows = jnp.arange(seq_len)
    return (
        (segments[:, None] == segments[None, :])
        & (key_rows[None, :] <= query_rows[:, None])
        & (query_rows[:, None] - key_rows[None, :] < WINDOW)
    )


MESH_ID = pl.DeviceIdType.MESH
GELU_A = 0.7978845608028654
GELU_B = 0.044715
TILE = 256


def remote(src, dst, send_sem, recv_sem, where):
    return pltpu.make_async_remote_copy(
        src_ref=src,
        dst_ref=dst,
        send_sem=send_sem,
        recv_sem=recv_sem,
        device_id=where,
        device_id_type=MESH_ID,
    )


def dot_nn(left, right):
    return lax.dot_general(
        left, right, (((1,), (0,)), ((), ())), preferred_element_type=jnp.float32
    )


def gelu_parts(gate):
    square = gate * gate
    bend = jnp.tanh(GELU_A * gate * (1.0 + GELU_B * square))
    half = 0.5 * (1.0 + bend)
    slope = half + 0.5 * gate * (1.0 - bend * bend) * GELU_A * (1.0 + 3.0 * GELU_B * square)
    return gate * half, slope


def add_rows(first, rest, out, count):
    def body(index, carry):
        step = pl.ds(pl.multiple_of(index * 32, 32), 32)
        total = first[step, :].astype(jnp.float32)
        for other in rest:
            total = total + other[step, :].astype(jnp.float32)
        out[step, :] = total.astype(out.dtype)
        return carry

    lax.fori_loop(0, count // 32, body, 0)


def ffn_kernel(
    z_size,
    main,
    own_ref,
    dy_hbm,
    w_hbm,
    gn_ref,
    mix_hbm,
    sums_hbm,
    n2,
    dy,
    w3,
    h3,
    left_t,
    gn_part,
    mix_buf,
    gn_y,
    gn_z,
    gn_s,
    c_in,
    x_in,
    load_sem,
    mix_sem,
    ag_y_send,
    ag_y_recv,
    ag_z_send,
    ag_z_recv,
    rs_y_send,
    rs_y_recv,
    rs_z_send,
    rs_z_recv,
    c_send,
    c_recv,
    x_send,
    x_recv,
    out_sem,
):
    own = own_ref.shape[0] // 2
    width = own_ref.shape[1]
    units = w3.shape[2]
    rows = c_in.shape[3]
    me_y, me_z = lax.axis_index("mp"), lax.axis_index("z")
    me_x, me_c = lax.axis_index("x"), lax.axis_index("c")
    mine = pl.ds(pl.multiple_of(me_y * own, own), own)
    theirs = pl.ds(pl.multiple_of((1 - me_y) * own, own), own)
    to_y, to_x, to_c = {"mp": 1 - me_y}, {"x": 1 - me_x}, {"c": 1 - me_c}

    def ahead(step):
        return lax.rem(me_z + step, z_size)

    def to_z(step):
        return {"z": ahead(step)}

    def row_block(z_at, x_at, c_at):
        return pl.ds(pl.multiple_of(((z_at * 2 + x_at) * 2 + c_at) * rows, rows), rows)

    loads = []
    for index in range(z_size):
        loads.append(pltpu.make_async_copy(dy_hbm.at[index], dy.at[index], load_sem.at[index]))
    for index in range(3):
        loads.append(
            pltpu.make_async_copy(w_hbm.at[index], w3.at[index], load_sem.at[z_size + index])
        )
    for load in loads:
        load.start()

    barrier = pltpu.get_barrier_semaphore()
    peers = [to_y, to_x, to_c] + [to_z(step) for step in range(1, z_size)]
    for where in peers:
        pl.semaphore_signal(barrier, inc=1, device_id=where, device_id_type=MESH_ID)
    pl.semaphore_wait(barrier, len(peers))

    def ag_y(index):
        block = n2.at[index, mine]
        return remote(block, block, ag_y_send.at[index], ag_y_recv.at[index], to_y)

    def ag_y_in(index):
        block = n2.at[index, theirs]
        return remote(block, block, ag_y_send.at[index], ag_y_recv.at[index], to_y)

    def ag_z(index):
        src = own_ref.at[mine] if index == 0 else n2.at[index, mine]
        return remote(
            src, n2.at[index + 1, mine], ag_z_send.at[index], ag_z_recv.at[index + 1], to_z(1)
        )

    def ag_z_in(index):
        block = n2.at[index, mine]
        return remote(block, block, ag_z_send.at[0], ag_z_recv.at[index], to_z(1))

    def forward(index):
        ag_z_in(index).wait_recv()
        if index < z_size - 1:
            ag_z(index).start()
        ag_y(index).start()

    ag_z(0).start()
    n2[0] = own_ref[...]

    mix_copies = []

    def chunk(index):
        if index:
            ag_y_in(index).wait_recv()
        if index >= 2:
            mix_copies[index - 2].wait()
        rows_at = pl.ds(index * 2 * own, 2 * own)

        def up_tile(tile, carry):
            cols = pl.ds(pl.multiple_of(tile * TILE, TILE), TILE)
            normed = n2[index]
            gate = dot_nn(normed, w3[0, :, cols])
            up_proj = dot_nn(normed, w3[1, :, cols])
            grad_hidden = dot_nn(dy[index], w3[2, :, cols])
            act, slope = gelu_parts(gate)
            at = lax.broadcasted_iota(jnp.int32, (1, TILE), 1) + tile * TILE
            low_at = main + 64 * lax.rem(me_z, 2)
            keep = (at < main) | ((at >= low_at) & (at < low_at + 64))
            act = jnp.where(keep, act, 0.0)
            slope = jnp.where(keep, slope, 0.0)
            h3[0, rows_at, cols] = (grad_hidden * up_proj * slope).astype(jnp.bfloat16)
            h3[1, rows_at, cols] = (grad_hidden * act).astype(jnp.bfloat16)
            h3[2, rows_at, cols] = (act * up_proj).astype(jnp.bfloat16)
            return carry

        lax.fori_loop(0, units // TILE, up_tile, 0)

        def down_tile(tile, carry):
            cols = pl.ds(pl.multiple_of(tile * TILE, TILE), TILE)
            gn_part[index, :, cols] = (
                matmul_nt(h3[0, rows_at, :], w3[0, cols, :])
                + matmul_nt(h3[1, rows_at, :], w3[1, cols, :])
            ).astype(jnp.bfloat16)
            mix_buf[index % 2, :, cols] = matmul_nt(h3[2, rows_at, :], w3[2, cols, :]).astype(
                jnp.bfloat16
            )
            return carry

        lax.fori_loop(0, width // TILE, down_tile, 0)
        copy = pltpu.make_async_copy(mix_buf.at[index % 2], mix_hbm.at[index], mix_sem.at[index])
        copy.start()
        mix_copies.append(copy)

    def rs_y(index):
        return remote(
            gn_part.at[index, theirs], gn_y.at[index], rs_y_send.at[index], rs_y_recv.at[index], to_y
        )

    def rs_z(index):
        return remote(
            gn_s.at[index - 1],
            gn_z.at[index - 1],
            rs_z_send.at[index],
            rs_z_recv.at[index - 1],
            to_z(1),
        )

    def rs_step(index):
        rs_y(index).wait_recv()
        slot = (index - 2) % z_size
        if index != 1:
            remote(
                gn_s.at[slot], gn_z.at[slot], rs_z_send.at[1], rs_z_recv.at[slot], to_z(1)
            ).wait_recv()

        def add_tile(tile, carry):
            cols = pl.ds(pl.multiple_of(tile * TILE, TILE), TILE)
            total = gn_part[index, mine, cols].astype(jnp.float32) + gn_y[index, :, cols].astype(
                jnp.float32
            )
            if index != 1:
                total = total + gn_z[slot, :, cols].astype(jnp.float32)
            if index == 0:
                gn_ref[:, cols] = total
            else:
                gn_s[index - 1, :, cols] = total.astype(jnp.bfloat16)
            return carry

        lax.fori_loop(0, width // TILE, add_tile, 0)
        if index != 0:
            rs_z(index).start()

    span = width // z_size

    def grads(step):
        at = pl.ds(pl.multiple_of(ahead(step) * span, 128), span)
        for kinds, source in (((0, 1), n2), ((2,), dy)):
            left_t[...] = source[:, :, at].reshape(z_size * 2 * own, span).T
            for kind in kinds:

                def tile_body(tile, carry, kind=kind):
                    cols = pl.ds(pl.multiple_of(tile * TILE, TILE), TILE)
                    w3[kind, at, cols] = dot_nn(left_t[...], h3[kind, :, cols]).astype(jnp.bfloat16)
                    return carry

                lax.fori_loop(0, units // TILE, tile_body, 0)
        for far in (1, 0):
            for kind in range(3):
                over_c(kind, step, far).start()

    def over_c(kind, step, far):
        x_at = 1 - me_x if far else me_x
        return remote(
            w3.at[kind, row_block(ahead(step), x_at, 1 - me_c)],
            c_in.at[kind, step, far],
            c_send.at[kind, step, far],
            c_recv.at[kind, step, far],
            to_c,
        )

    def over_x(kind):
        return remote(
            w3.at[kind, row_block(ahead(1), 1 - me_x, me_c)],
            x_in.at[kind],
            x_send.at[kind],
            x_recv.at[kind],
            to_x,
        )

    out_copies = []

    def keep(kind, step, far, block):
        copy = pltpu.make_async_copy(
            block, sums_hbm.at[kind, step, far], out_sem.at[kind, step, far]
        )
        copy.start()
        out_copies.append(copy)

    def core_sums(step):
        for far in (1, 0):
            for kind in range(3):
                over_c(kind, step, far).wait_recv()
                x_at = 1 - me_x if far else me_x
                block = w3.at[kind, row_block(ahead(step), x_at, me_c)]
                add_rows(block, [c_in.at[kind, step, far]], block, rows)
                if step != 1:
                    keep(kind, step, far, block)
                elif far:
                    over_x(kind).start()

    def first_sums():
        for kind in range(3):
            over_x(kind).wait_recv()
            block = w3.at[kind, row_block(ahead(1), me_x, me_c)]
            add_rows(block, [x_in.at[kind]], block, rows)
            keep(kind, 1, 0, block)

    forward(1)
    for load in loads:
        load.wait()
    chunk(0)
    rs_y(0).start()
    forward(2)
    chunk(1)
    rs_y(1).start()
    forward(3)
    chunk(2)
    rs_y(2).start()
    rs_step(1)
    chunk(3)
    rs_y(3).start()
    rs_step(2)
    grads(1)
    grads(2)
    core_sums(1)
    rs_step(3)
    grads(3)
    core_sums(2)
    grads(0)
    core_sums(3)
    rs_step(0)
    core_sums(0)
    first_sums()

    for copy in mix_copies[2:] + out_copies:
        copy.wait()
    for index in range(z_size):
        if index:
            ag_y(index).wait_send()
        rs_y(index).wait_send()
        if index < z_size - 1:
            ag_z(index).wait_send()
        if index:
            rs_z(index).wait_send()
        for kind in range(3):
            over_c(kind, index, 0).wait_send()
            over_c(kind, index, 1).wait_send()
            if index == 1:
                over_x(kind).wait_send()


def ffn_call(normed, grad_all, weights, rows, main):
    z_size = lax.axis_size("z")
    pair, width = normed.shape
    units = weights.shape[2]
    own = pair // 2
    wide = lambda *lead: pltpu.VMEM((*lead, width), jnp.bfloat16)
    dma = lambda *lead: pltpu.SemaphoreType.DMA(lead)
    vmem = pl.BlockSpec(memory_space=pltpu.VMEM)
    hbm = pl.BlockSpec(memory_space=pl.ANY)
    return pl.pallas_call(
        functools.partial(ffn_kernel, z_size, main),
        out_shape=(
            jax.ShapeDtypeStruct((own, width), jnp.float32),
            jax.ShapeDtypeStruct((z_size, pair, width), jnp.bfloat16),
            jax.ShapeDtypeStruct((3, z_size, 2, rows, units), jnp.bfloat16),
        ),
        in_specs=[vmem, hbm, hbm],
        out_specs=(vmem, hbm, hbm),
        scratch_shapes=[
            wide(z_size, pair),
            wide(z_size, pair),
            pltpu.VMEM(weights.shape, jnp.bfloat16),
            pltpu.VMEM((3, z_size * pair, units), jnp.bfloat16),
            pltpu.VMEM((width // z_size, z_size * pair), jnp.bfloat16),
            wide(z_size, pair),
            wide(2, pair),
            wide(z_size, own),
            wide(z_size - 1, own),
            wide(z_size - 1, own),
            pltpu.VMEM((3, z_size, 2, rows, units), jnp.bfloat16),
            pltpu.VMEM((3, rows, units), jnp.bfloat16),
            dma(z_size + 3),
            dma(z_size),
            dma(z_size),
            dma(z_size),
            dma(z_size),
            dma(z_size),
            dma(z_size),
            dma(z_size),
            dma(z_size),
            dma(z_size),
            dma(3, z_size, 2),
            dma(3, z_size, 2),
            dma(3),
            dma(3),
            dma(3, z_size, 2),
        ],
        compiler_params=pltpu.CompilerParams(
            collective_id=0, has_side_effects=True, vmem_limit_bytes=VMEM_BYTES
        ),
        cost_estimate=pl.CostEstimate(
            flops=18 * z_size * pair * width * units,
            bytes_accessed=4 * weights.size + 12 * z_size * pair * width,
            transcendentals=z_size * pair * units,
        ),
    )(normed, grad_all, weights)


def spin(values, table):
    first = values[:, : values.shape[1] // 2]
    turned = first * table[0] + pltpu.roll(first, first.shape[1] // 2, 1) * table[1]
    return jnp.concatenate([turned, values[:, values.shape[1] // 2 :]], axis=1)


def spin_back(values, table):
    first = values[:, : values.shape[1] // 2]
    turned = first * table[0] - pltpu.roll(first, first.shape[1] // 2, 1) * table[1]
    return jnp.concatenate([turned, values[:, values.shape[1] // 2 :]], axis=1)


def head_probs(rotated, keys, allowed):
    scores = jnp.where(allowed > 0.5, matmul_nt(rotated, keys), masked_score)
    weights = jnp.exp(scores - jnp.max(scores, axis=-1, keepdims=True))
    return weights / jnp.sum(weights, axis=-1, keepdims=True)


def ragged_split(columns, parts):
    main = columns // parts // 128 * 128
    return main, main + 128


def pre_kernel(
    z_size,
    tok_ref,
    kvg_ref,
    table_ref,
    allow_ref,
    cot_hbm,
    wq_hbm,
    wo_hbm,
    wg_hbm,
    wu_hbm,
    wd_hbm,
    n1_ref,
    rot_ref,
    key_ref,
    val_ref,
    att_ref,
    mid_ref,
    n2_ref,
    gain_ref,
    kv_out,
    wq_out,
    wo_out,
    w3_out,
    dy_out,
    kv_w,
    q_w,
    o_w,
    tok,
    part,
    part_y,
    y_send,
    y_recv,
    az_send,
    az_recv,
    ax_send,
    ax_recv,
    ac_send,
    ac_recv,
    fz_send,
    fz_recv,
    fx_send,
    fx_recv,
    fc_send,
    fc_recv,
    dz_send,
    dz_recv,
    dy_send,
    dy_recv,
    local_sem,
):
    me_z, me_x = lax.axis_index("z"), lax.axis_index("x")
    me_c, me_y = lax.axis_index("c"), lax.axis_index("mp")
    own, width = tok_ref.shape
    rows = wq_hbm.shape[0]
    half_rows = kvg_ref.shape[0]
    head = key_ref.shape[1]
    main, units = ragged_split(wg_hbm.shape[1], z_size)
    to_y, to_x, to_c = {"mp": 1 - me_y}, {"x": 1 - me_x}, {"c": 1 - me_c}

    def to_z(step):
        return {"z": lax.rem(me_z + step, z_size)}

    def from_z(step):
        return lax.rem(me_z - step + z_size, z_size)

    def row_block(step, x_at, c_at):
        start = ((from_z(step) * 2 + x_at) * 2 + c_at) * rows
        return pl.ds(pl.multiple_of(start, rows), rows)

    mine = pl.ds(pl.multiple_of(me_y * own, own), own)
    theirs = pl.ds(pl.multiple_of((1 - me_y) * own, own), own)
    bufs = (kv_w, q_w, o_w)
    inputs = (None, wq_hbm, wo_hbm)

    locals_ = []

    def local(src, dst):
        copy = pltpu.make_async_copy(src, dst, local_sem.at[len(locals_)])
        copy.start()
        locals_.append(copy)
        return copy

    here = row_block(0, me_x, me_c)
    own_q = local(wq_hbm, q_w.at[here])
    own_o = local(wo_hbm, o_w.at[here])
    ffn_in = (wg_hbm, wu_hbm, wd_hbm)

    def pieces(target):
        yield pl.ds(pl.multiple_of(target * main, 128), main), pl.ds(0, main)
        tail = (z_size * main) + (target // 2) * 128
        yield pl.ds(pl.multiple_of(tail, 128), 128), pl.ds(main, 128)

    own_f = []
    for kind in range(3):
        for src, dst in pieces(me_z):
            own_f.append(local(ffn_in[kind].at[:, src], w3_out.at[kind, here, dst]))
    own_d = local(cot_hbm, dy_out.at[0, mine])

    barrier = pltpu.get_barrier_semaphore()
    peers = [to_y, to_x, to_c] + [to_z(step) for step in range(1, z_size)]
    for where in peers:
        pl.semaphore_signal(barrier, inc=1, device_id=where, device_id_type=MESH_ID)
    pl.semaphore_wait(barrier, len(peers))

    kv_mine = pl.ds(pl.multiple_of(here.start + me_y * half_rows, half_rows), half_rows)
    kv_theirs = pl.ds(pl.multiple_of(here.start + (1 - me_y) * half_rows, half_rows), half_rows)
    kv_y = remote(kvg_ref, kv_w.at[kv_mine], y_send.at[0], y_recv.at[0], to_y)
    kv_y_in = remote(kvg_ref, kv_w.at[kv_theirs], y_send.at[0], y_recv.at[0], to_y)
    tok_y = remote(tok_ref, tok.at[mine], y_send.at[1], y_recv.at[1], to_y)
    tok_y_in = remote(tok_ref, tok.at[theirs], y_send.at[1], y_recv.at[1], to_y)
    part_out = remote(part.at[theirs], part_y, y_send.at[2], y_recv.at[2], to_y)
    n2_y = remote(n2_ref.at[mine], n2_ref.at[mine], y_send.at[3], y_recv.at[3], to_y)
    n2_y_in = remote(n2_ref.at[theirs], n2_ref.at[theirs], y_send.at[3], y_recv.at[3], to_y)

    def source(kind, step):
        if step == 0 and kind:
            return inputs[kind]
        return bufs[kind].at[row_block(step, me_x, me_c)]

    def a_z(kind, step):
        return remote(
            source(kind, step),
            bufs[kind].at[row_block(step, me_x, me_c)],
            az_send.at[kind, step],
            az_recv.at[kind, step + 1],
            to_z(1),
        )

    def a_z_in(kind, step):
        block = bufs[kind].at[row_block(step, me_x, me_c)]
        return remote(block, block, az_send.at[kind, 0], az_recv.at[kind, step], to_z(1))

    def a_x(kind, step):
        return remote(
            source(kind, step),
            bufs[kind].at[row_block(step, me_x, me_c)],
            ax_send.at[kind, step],
            ax_recv.at[kind, step],
            to_x,
        )

    def a_x_in(kind, step):
        block = bufs[kind].at[row_block(step, 1 - me_x, me_c)]
        return remote(block, block, ax_send.at[kind, step], ax_recv.at[kind, step], to_x)

    def a_c(kind, step, far):
        x_at = 1 - me_x if far else me_x
        block = bufs[kind].at[row_block(step, x_at, me_c)]
        src = block if far else source(kind, step)
        slot = step + z_size * far
        return remote(src, block, ac_send.at[kind, slot], ac_recv.at[kind, slot], to_c)

    def a_c_in(kind, step, far):
        x_at = 1 - me_x if far else me_x
        block = bufs[kind].at[row_block(step, x_at, 1 - me_c)]
        slot = step + z_size * far
        return remote(block, block, ac_send.at[kind, slot], ac_recv.at[kind, slot], to_c)

    def f_z(kind, step):
        target = lax.rem(me_z + step, z_size)
        return [
            remote(
                ffn_in[kind].at[:, src],
                w3_out.at[kind, here, dst],
                fz_send.at[kind, step, index],
                fz_recv.at[kind, step, index],
                to_z(step),
            )
            for index, (src, dst) in enumerate(pieces(target))
        ]

    def f_z_in(kind, step):
        block = row_block(step, me_x, me_c)
        return [
            remote(
                w3_out.at[kind, block, dst],
                w3_out.at[kind, block, dst],
                fz_send.at[kind, step, index],
                fz_recv.at[kind, step, index],
                to_z(step),
            )
            for index, (_, dst) in enumerate(pieces(me_z))
        ]

    def f_x(kind, step):
        block = w3_out.at[kind, row_block(step, me_x, me_c)]
        return remote(block, block, fx_send.at[kind, step], fx_recv.at[kind, step], to_x)

    def f_x_in(kind, step):
        block = w3_out.at[kind, row_block(step, 1 - me_x, me_c)]
        return remote(block, block, fx_send.at[kind, step], fx_recv.at[kind, step], to_x)

    def f_c(kind, step, far):
        block = w3_out.at[kind, row_block(step, 1 - me_x if far else me_x, me_c)]
        slot = step + z_size * far
        return remote(block, block, fc_send.at[kind, slot], fc_recv.at[kind, slot], to_c)

    def f_c_in(kind, step, far):
        block = w3_out.at[kind, row_block(step, 1 - me_x if far else me_x, 1 - me_c)]
        slot = step + z_size * far
        return remote(block, block, fc_send.at[kind, slot], fc_recv.at[kind, slot], to_c)

    def d_source(step):
        return cot_hbm if step == 0 else dy_out.at[step, mine]

    def d_z(step):
        return remote(
            d_source(step), dy_out.at[step + 1, mine], dz_send.at[step], dz_recv.at[step + 1], to_z(1)
        )

    def d_z_in(step):
        block = dy_out.at[step, mine]
        return remote(block, block, dz_send.at[0], dz_recv.at[step], to_z(1))

    def d_y(step):
        return remote(
            d_source(step), dy_out.at[step, mine], dy_send.at[step], dy_recv.at[step], to_y
        )

    def d_y_in(step):
        block = dy_out.at[step, theirs]
        return remote(block, block, dy_send.at[step], dy_recv.at[step], to_y)

    kv_y.start()
    tok_y.start()
    for kind in (1, 2):
        a_z(kind, 0).start()
        a_x(kind, 0).start()
        a_c(kind, 0, 0).start()
    kv_w[kv_mine, :] = kvg_ref[...]
    tok[mine, :] = tok_ref[...]
    kv_y_in.wait_recv()
    a_z(0, 0).start()
    a_x(0, 0).start()
    a_c(0, 0, 0).start()
    d_y(0).start()
    for step in range(1, z_size):
        for kind in (1, 0, 2):
            a_z_in(kind, step).wait_recv()
            if step < z_size - 1:
                a_z(kind, step).start()
            a_x(kind, step).start()
            a_c(kind, step, 0).start()
        if step == z_size - 2:
            for copy in own_f:
                copy.wait()
            d_z(0).start()
            for kind in range(3):
                for away in (1, 3, 2):
                    for copy in f_z(kind, away):
                        copy.start()
        for kind in (1, 0, 2):
            a_x_in(kind, step - 1).wait_recv()
            a_c(kind, step - 1, 1).start()
    for kind in range(3):
        f_x(kind, 0).start()
        f_c(kind, 0, 0).start()

    def hand_on(kind, step):
        for copy in f_z_in(kind, step):
            copy.wait_recv()
        f_x(kind, step).start()
        f_c(kind, step, 0).start()

    def cross(kind, step):
        f_x_in(kind, step).wait_recv()
        f_c(kind, step, 1).start()

    def pass_cotangent(step):
        d_z_in(step).wait_recv()
        if step < z_size - 1:
            d_z(step).start()
        d_y(step).start()

    pass_cotangent(1)
    for kind in (1, 0, 2):
        a_x_in(kind, z_size - 1).wait_recv()
        a_c(kind, z_size - 1, 1).start()
    hand_on(0, 1)
    tok_y_in.wait_recv()
    own_q.wait()
    own_o.wait()
    for kind in (0, 1):
        for step in range(z_size):
            for far in range(2):
                a_c_in(kind, step, far).wait_recv()

    gains = kv_w[:, 2 * head :].astype(jnp.float32).T[:8, :]
    gain_ref[...] = gains

    def norm_rows(index, carry):
        at = pl.ds(pl.multiple_of(index * 32, 32), 32)
        values = tok[at, :].astype(jnp.float32)
        scale = lax.rsqrt(jnp.mean(values * values, axis=-1, keepdims=True) + epsilon)
        n1_ref[at, :] = (values * scale * gain_ref[0:1, :]).astype(jnp.bfloat16)
        return carry

    lax.fori_loop(0, 2 * own // 32, norm_rows, 0)
    hand_on(0, 3)
    table = (table_ref[0], table_ref[1])
    key_ref[...] = spin(dot_nn(n1_ref[...], kv_w[:, :head]), table).astype(jnp.bfloat16)
    val_ref[...] = dot_nn(n1_ref[...], kv_w[:, head : 2 * head]).astype(jnp.bfloat16)
    hand_on(0, 2)
    head_scale = head ** (-0.5)
    heads = att_ref.shape[1] // head

    def attend(index):
        cols = pl.ds(index * head, head)
        query = dot_nn(n1_ref[...], q_w[:, cols])
        rotated = (spin(query, table) * head_scale).astype(jnp.bfloat16)
        rot_ref[:, cols] = rotated
        probs = head_probs(rotated, key_ref[...], allow_ref[...]).astype(jnp.bfloat16)
        att_ref[:, cols] = dot_nn(probs, val_ref[...]).astype(jnp.bfloat16)

    tasks = [
        lambda: cross(0, 0),
        lambda: hand_on(1, 1),
        lambda: pass_cotangent(2),
        lambda: hand_on(1, 3),
        lambda: cross(1, 0),
    ]
    for index in range(heads):
        attend(index)
        if index < len(tasks):
            tasks[index]()
    for step in range(z_size):
        for far in range(2):
            a_c_in(2, step, far).wait_recv()
    saves = [
        local(kv_w, kv_out),
        local(q_w, wq_out),
        local(o_w, wo_out),
    ]
    span = width // 4

    def project(index, carry):
        cols = pl.ds(pl.multiple_of(index * span, span), span)
        part[:, cols] = matmul_nt(att_ref[...], o_w[cols, :]).astype(jnp.bfloat16)
        return carry

    lax.fori_loop(0, 4, project, 0)
    part_out.start()
    hand_on(1, 2)
    cross(2, 0)
    cross(0, 1)
    hand_on(2, 1)
    part_out.wait_recv()

    def middle(index, carry):
        at = pl.ds(pl.multiple_of(index * 32, 32), 32)
        there = pl.ds(pl.multiple_of(me_y * own + index * 32, 32), 32)
        values = (
            tok_ref[at, :].astype(jnp.float32)
            + part[there, :].astype(jnp.float32)
            + part_y[at, :].astype(jnp.float32)
        )
        mid_ref[at, :] = values
        scale = lax.rsqrt(jnp.mean(values * values, axis=-1, keepdims=True) + epsilon)
        n2_ref[there, :] = (values * scale * gain_ref[1:2, :]).astype(jnp.bfloat16)
        return carry

    lax.fori_loop(0, own // 32, middle, 0)
    n2_y.start()
    cross(0, 3)
    hand_on(2, 3)
    pass_cotangent(3)
    cross(0, 2)
    hand_on(2, 2)
    for kind in (1, 2):
        for step in (1, 3, 2):
            cross(kind, step)
    for kind in range(3):
        for step in range(z_size):
            for far in range(2):
                f_c_in(kind, step, far).wait_recv()
    for step in range(z_size):
        d_y_in(step).wait_recv()
    n2_y_in.wait_recv()

    kv_y.wait_send()
    tok_y.wait_send()
    part_out.wait_send()
    n2_y.wait_send()
    own_d.wait()
    for copy in saves:
        copy.wait()
    for step in range(z_size):
        d_y(step).wait_send()
        if step < z_size - 1:
            d_z(step).wait_send()
        for kind in range(3):
            if step < z_size - 1:
                a_z(kind, step).wait_send()
            if step:
                for copy in f_z(kind, step):
                    copy.wait_send()
            a_x(kind, step).wait_send()
            f_x(kind, step).wait_send()
            for far in range(2):
                a_c(kind, step, far).wait_send()
                f_c(kind, step, far).wait_send()


def pre_call(tokens, kv_gains, table, allowed, cotangent, w_query, w_out, ffn):
    z_size = lax.axis_size("z")
    own, width = tokens.shape
    seq = 2 * own
    rows, cols = w_query.shape
    head = table.shape[2] * 2
    units = ragged_split(ffn[0].shape[1], z_size)[1]
    low = lambda *dims: jax.ShapeDtypeStruct(dims, jnp.bfloat16)
    full = lambda *dims: jax.ShapeDtypeStruct(dims, jnp.float32)
    dma = lambda *lead: pltpu.SemaphoreType.DMA(lead)
    vmem = pl.BlockSpec(memory_space=pltpu.VMEM)
    hbm = pl.BlockSpec(memory_space=pl.ANY)
    wide = lambda *lead: pltpu.VMEM((*lead, width), jnp.bfloat16)
    return pl.pallas_call(
        functools.partial(pre_kernel, z_size),
        out_shape=(
            low(seq, width),
            low(seq, cols),
            low(seq, head),
            low(seq, head),
            low(seq, cols),
            full(own, width),
            low(seq, width),
            full(8, width),
            low(width, kv_gains.shape[1]),
            low(width, cols),
            low(width, cols),
            low(3, width, units),
            low(z_size, seq, width),
        ),
        in_specs=[vmem] * 4 + [hbm] * 6,
        out_specs=(vmem,) * 8 + (hbm,) * 5,
        scratch_shapes=[
            pltpu.VMEM((width, kv_gains.shape[1]), jnp.bfloat16),
            pltpu.VMEM((width, cols), jnp.bfloat16),
            pltpu.VMEM((width, cols), jnp.bfloat16),
            wide(seq),
            wide(seq),
            wide(own),
            dma(4),
            dma(4),
            dma(3, z_size),
            dma(3, z_size),
            dma(3, z_size),
            dma(3, z_size),
            dma(3, 2 * z_size),
            dma(3, 2 * z_size),
            dma(3, z_size, 2),
            dma(3, z_size, 2),
            dma(3, z_size),
            dma(3, z_size),
            dma(3, 2 * z_size),
            dma(3, 2 * z_size),
            dma(z_size),
            dma(z_size),
            dma(z_size),
            dma(z_size),
            dma(16),
        ],
        compiler_params=pltpu.CompilerParams(
            collective_id=1, has_side_effects=True, vmem_limit_bytes=VMEM_BYTES
        ),
        cost_estimate=pl.CostEstimate(
            flops=8 * seq * width * cols,
            bytes_accessed=8 * width * (cols + units),
            transcendentals=seq * seq * cols // head,
        ),
    )(tokens, kv_gains, table, allowed, cotangent, w_query, w_out, *ffn)


def norm_back(values, gain, upstream):
    scale = lax.rsqrt(jnp.mean(values * values, axis=-1, keepdims=True) + epsilon)
    normed = values * scale
    pulled = gain * upstream
    back = scale * (pulled - normed * jnp.mean(normed * pulled, axis=-1, keepdims=True))
    return back, jnp.sum(upstream * normed, axis=0, keepdims=True)


def post_kernel(
    z_size,
    mid_ref,
    tok_ref,
    cot_ref,
    gain_ref,
    n1_ref,
    rot_ref,
    key_ref,
    val_ref,
    att_ref,
    table_ref,
    allow_ref,
    kv_hbm,
    wq_hbm,
    wo_hbm,
    mix_hbm,
    gn_hbm,
    sums_hbm,
    mixed_ref,
    tgrad_ref,
    gsum_ref,
    kvg_ref,
    qg_ref,
    og_ref,
    ffn_out,
    kv_w,
    q_w,
    o_w,
    o_part,
    gm,
    gm_f,
    gq,
    gkv,
    kv_sum,
    back_y,
    mix_y,
    mix_z,
    mix_s,
    o_c,
    o_x,
    o_z,
    q_c,
    q_x,
    q_z,
    kv_y,
    kv_c,
    kv_x,
    kv_z,
    gain_own,
    gain_in,
    ffn_in,
    ffn_own,
    load_sem,
    own_sem,
    out_sem,
    fx_send,
    fx_recv,
    fz_send,
    fz_recv,
    y_send,
    y_recv,
    my_send,
    my_recv,
    mz_send,
    mz_recv,
    wc_send,
    wc_recv,
    wx_send,
    wx_recv,
    wz_send,
    wz_recv,
    kc_send,
    kc_recv,
    kz_send,
    kz_recv,
    g_send,
    g_recv,
):
    me_z, me_x = lax.axis_index("z"), lax.axis_index("x")
    me_c, me_y = lax.axis_index("c"), lax.axis_index("mp")
    own, width = tok_ref.shape
    seq = 2 * own
    head = key_ref.shape[1]
    cols_here = att_ref.shape[1]
    heads = cols_here // head
    rows = qg_ref.shape[0]
    span = width // z_size
    mine = pl.ds(pl.multiple_of(me_y * own, own), own)
    theirs = pl.ds(pl.multiple_of((1 - me_y) * own, own), own)
    to_y, to_x, to_c = {"mp": 1 - me_y}, {"x": 1 - me_x}, {"c": 1 - me_c}
    head_scale = head ** (-0.5)

    def behind(step):
        return lax.rem(me_z - step + z_size, z_size)

    def to_z(step):
        return {"z": lax.rem(me_z + step, z_size)}

    def row_block(step, x_at, c_at):
        start = ((behind(step) * 2 + x_at) * 2 + c_at) * rows
        return pl.ds(pl.multiple_of(start, rows), rows)

    loads = [
        pltpu.make_async_copy(wo_hbm, o_w, load_sem.at[0]),
        pltpu.make_async_copy(wq_hbm, q_w, load_sem.at[1]),
        pltpu.make_async_copy(
            kv_hbm.at[:, :, :, :, :, pl.ds(0, 2 * head)], kv_w, load_sem.at[2]
        ),
    ]
    for step in range(z_size):
        loads.append(
            pltpu.make_async_copy(mix_hbm.at[step, mine], mix_s.at[step], load_sem.at[3 + step])
        )
    gn_load = pltpu.make_async_copy(gn_hbm, gm_f, load_sem.at[3 + z_size])
    gn_load.start()
    for load in loads:
        load.start()

    barrier = pltpu.get_barrier_semaphore()
    peers = [to_y, to_x, to_c] + [to_z(step) for step in range(1, z_size)]
    for where in peers:
        pl.semaphore_signal(barrier, inc=1, device_id=where, device_id_type=MESH_ID)
    pl.semaphore_wait(barrier, len(peers))

    tasks = [(step, kind) for step in (2, 3, 0) for kind in range(3)]

    def f_x(index):
        step, kind = tasks[index]
        return remote(
            sums_hbm.at[kind, step, 1],
            ffn_in.at[index],
            fx_send.at[index],
            fx_recv.at[index],
            to_x,
        )

    def f_own(index):
        step, kind = tasks[index]
        return pltpu.make_async_copy(
            sums_hbm.at[kind, step, 0], ffn_own.at[index % 2], own_sem.at[index % 2]
        )

    def f_z(step, kind):
        if step == 1:
            src = sums_hbm.at[kind, 1, 0]
        else:
            src = ffn_in.at[tasks.index((step, kind))]
        return remote(
            src, ffn_out.at[kind, step], fz_send.at[kind, step], fz_recv.at[kind, step], to_z(step)
        )

    own_out = []

    def tick(index):
        step, kind = tasks[index]
        f_x(index).wait_recv()
        f_own(index).wait()
        block = ffn_in.at[index]
        add_rows(block, [ffn_own.at[index % 2]], block, rows)
        if index + 2 < len(tasks):
            f_own(index + 2).start()
        if step:
            f_z(step, kind).start()
        else:
            copy = pltpu.make_async_copy(block, ffn_out.at[kind, 0], out_sem.at[kind])
            copy.start()
            own_out.append(copy)

    f_own(0).start()
    f_own(1).start()
    for index in range(len(tasks)):
        f_x(index).start()
    for kind in range(3):
        f_z(1, kind).start()

    gn_load.wait()

    def mid_rows(index, total):
        at = pl.ds(pl.multiple_of(index * 32, 32), 32)
        grad, gain_part = norm_back(mid_ref[at, :], gain_ref[1:2, :], gm_f[at, :])
        grad = grad + cot_ref[at, :].astype(jnp.float32)
        gm_f[at, :] = grad
        gm[pl.ds(pl.multiple_of(me_y * own + index * 32, 32), 32), :] = grad.astype(jnp.bfloat16)
        return total + gain_part

    ffn_gain_part = lax.fori_loop(
        0, own // 32, mid_rows, jnp.zeros((1, width), jnp.float32)
    )
    gm_y = remote(gm.at[mine], gm.at[mine], y_send.at[0], y_recv.at[0], to_y)
    gm_y_in = remote(gm.at[theirs], gm.at[theirs], y_send.at[0], y_recv.at[0], to_y)
    gm_y.start()

    def mix_over_y(step):
        return remote(
            mix_hbm.at[step, theirs], mix_y.at[step], my_send.at[step], my_recv.at[step], to_y
        )

    def mix_over_z(step):
        return remote(
            mix_s.at[step], mix_z.at[step - 1], mz_send.at[step], mz_recv.at[step - 1], to_z(1)
        )

    def mix_step(step):
        mix_over_y(step).wait_recv()
        slot = (step - 2) % z_size
        others = [mix_y.at[step]]
        if step != 1:
            remote(
                mix_s.at[1], mix_z.at[slot], mz_send.at[1], mz_recv.at[slot], to_z(1)
            ).wait_recv()
            others.append(mix_z.at[slot])
        if step:
            add_rows(mix_s.at[step], others, mix_s.at[step], own)
            mix_over_z(step).start()
        else:
            add_rows(mid_ref, [mix_s.at[0], *others], mixed_ref, own)

    for step in (1, 2, 3, 0):
        mix_over_y(step).start()

    kinds = ((o_part, o_c, o_x, o_z, og_ref), (o_w, q_c, q_x, q_z, qg_ref))

    def w_c(kind, step, far):
        x_at = 1 - me_x if far else me_x
        return remote(
            kinds[kind][0].at[row_block(step, x_at, 1 - me_c)],
            kinds[kind][1].at[step, far],
            wc_send.at[kind, step, far],
            wc_recv.at[kind, step, far],
            to_c,
        )

    def w_x(kind, step):
        return remote(
            kinds[kind][0].at[row_block(step, 1 - me_x, me_c)],
            kinds[kind][2].at[step],
            wx_send.at[kind, step],
            wx_recv.at[kind, step],
            to_x,
        )

    def w_z(kind, step):
        return remote(
            kinds[kind][0].at[row_block(step, me_x, me_c)],
            kinds[kind][3].at[step - 1],
            wz_send.at[kind, step],
            wz_recv.at[kind, step - 1],
            to_z(1),
        )

    def w_x_stage(kind, step):
        w_c(kind, step, 1).wait_recv()
        block = kinds[kind][0].at[row_block(step, 1 - me_x, me_c)]
        add_rows(block, [kinds[kind][1].at[step, 1]], block, rows)
        w_x(kind, step).start()

    def w_z_stage(kind, step):
        part, from_c, from_x, from_z, result = kinds[kind]
        w_c(kind, step, 0).wait_recv()
        w_x(kind, step).wait_recv()
        others = [from_c.at[step, 0], from_x.at[step]]
        slot = (step - 2) % z_size
        if step != 1:
            remote(
                from_z.at[slot],
                from_z.at[slot],
                wz_send.at[kind, 1],
                wz_recv.at[kind, slot],
                to_z(1),
            ).wait_recv()
            others.append(from_z.at[slot])
        block = part.at[row_block(step, me_x, me_c)]
        if step:
            add_rows(block, others, block, rows)
            w_z(kind, step).start()
        else:
            add_rows(block, others, result, rows)

    def w_product(kind, step, left, right):
        at = pl.ds(pl.multiple_of(behind(step) * span, 128), span)
        turned = left[:, at].T

        def tile_body(tile, carry):
            cols = pl.ds(pl.multiple_of(tile * TILE, TILE), TILE)
            kinds[kind][0][at, cols] = dot_nn(turned, right[:, cols]).astype(jnp.bfloat16)
            return carry

        lax.fori_loop(0, cols_here // TILE, tile_body, 0)
        for far in (1, 0):
            w_c(kind, step, far).start()

    order = (1, 2, 3, 0)
    tick(0)
    tick(1)
    gm_y_in.wait_recv()
    w_product(0, 1, gm, att_ref)
    w_product(0, 2, gm, att_ref)
    w_x_stage(0, 1)
    w_product(0, 3, gm, att_ref)
    w_x_stage(0, 2)
    tick(2)
    w_product(0, 0, gm, att_ref)
    w_x_stage(0, 3)
    for load in loads:
        load.wait()

    kv_sum[...] = jnp.zeros(kv_sum.shape, jnp.float32)
    table = (table_ref[0], table_ref[1])

    def attend_back(index):
        cols = pl.ds(index * head, head)
        grad_vals = dot_nn(gm[...], o_w[:, cols]).astype(jnp.bfloat16)
        rotated = rot_ref[:, cols]
        probs = head_probs(rotated, key_ref[...], allow_ref[...])
        grad_probs = matmul_nt(grad_vals, val_ref[...])
        delta = jnp.sum(probs * grad_probs, axis=-1, keepdims=True)
        grad_scores = (probs * (grad_probs - delta)).astype(jnp.bfloat16)
        grad_rot = dot_nn(grad_scores, key_ref[...])
        gq[:, cols] = (spin_back(grad_rot, table) * head_scale).astype(jnp.bfloat16)
        kv_sum[0] += matmul_tn(grad_scores, rotated)
        kv_sum[1] += matmul_tn(probs.astype(jnp.bfloat16), grad_vals)

    for index in range(heads):
        attend_back(index)
        if index == 0:
            w_x_stage(0, 0)
        if 3 + index < 8:
            tick(3 + index)
    gkv[:, :head] = spin_back(kv_sum[0], table).astype(jnp.bfloat16)
    gkv[:, head:] = kv_sum[1].astype(jnp.bfloat16)

    w_product(1, 1, n1_ref, gq)
    mix_step(1)
    w_product(1, 2, n1_ref, gq)
    w_x_stage(1, 1)
    w_z_stage(0, 1)
    w_product(1, 3, n1_ref, gq)
    w_x_stage(1, 2)
    w_product(1, 0, n1_ref, gq)
    w_x_stage(1, 3)
    tick(8)
    w_x_stage(1, 0)
    mix_step(2)

    gm_y.wait_send()
    back = gm
    def input_tile(index, carry):
        at = pl.ds(pl.multiple_of(index * span, 128), span)
        back[:, at] = (
            matmul_nt(gq[...], q_w[at, :]) + matmul_nt(gkv[...], kv_w[index].reshape(span, 2 * head))
        ).astype(jnp.bfloat16)
        return carry

    lax.fori_loop(0, z_size, input_tile, 0)
    back_out = remote(back.at[theirs], back_y, y_send.at[1], y_recv.at[1], to_y)
    back_out.start()

    kv_part = kv_w

    def kv_tile(index, carry):
        at = pl.ds(pl.multiple_of(index * span, 128), span)
        product = dot_nn(n1_ref[:, at].T, gkv[...]).astype(jnp.bfloat16)
        kv_part[index] = product.reshape(kv_part.shape[1:])
        return carry

    lax.fori_loop(0, z_size, kv_tile, 0)
    kv_over_y = remote(kv_part.at[:, :, :, 1 - me_y], kv_y, y_send.at[2], y_recv.at[2], to_y)
    kv_over_y.start()
    w_z_stage(0, 2)
    mix_step(3)
    kv_over_y.wait_recv()

    def kv_add_y(index, carry):
        for x_at in range(2):
            for c_at in range(2):
                block = kv_part.at[index, x_at, c_at, me_y]
                block[...] = (
                    block[...].astype(jnp.float32) + kv_y[index, x_at, c_at].astype(jnp.float32)
                ).astype(jnp.bfloat16)
        return carry

    lax.fori_loop(0, z_size, kv_add_y, 0)
    kv_over_c = remote(
        kv_part.at[:, :, 1 - me_c, me_y], kv_c, kc_send.at[0], kc_recv.at[0], to_c
    )
    kv_over_c.start()
    w_z_stage(0, 3)
    w_z_stage(1, 1)
    kv_over_c.wait_recv()

    def kv_add_c(index, carry):
        for x_at in range(2):
            block = kv_part.at[index, x_at, me_c, me_y]
            block[...] = (
                block[...].astype(jnp.float32) + kv_c[index, x_at].astype(jnp.float32)
            ).astype(jnp.bfloat16)
        return carry

    lax.fori_loop(0, z_size, kv_add_c, 0)
    kv_over_x = remote(
        kv_part.at[:, 1 - me_x, me_c, me_y], kv_x, kc_send.at[1], kc_recv.at[1], to_x
    )
    kv_over_x.start()

    back_out.wait_recv()

    def input_rows(index, total):
        at = pl.ds(pl.multiple_of(index * 32, 32), 32)
        there = pl.ds(pl.multiple_of(me_y * own + index * 32, 32), 32)
        upstream = back[there, :].astype(jnp.float32) + back_y[at, :].astype(jnp.float32)
        grad, gain_part = norm_back(
            tok_ref[at, :].astype(jnp.float32), gain_ref[0:1, :], upstream
        )
        tgrad_ref[at, :] = (gm_f[at, :] + grad).astype(jnp.bfloat16)
        return total + gain_part

    attn_gain_part = lax.fori_loop(
        0, own // 32, input_rows, jnp.zeros((1, width), jnp.float32)
    )
    gain_own[0, 0:1, :] = attn_gain_part
    gain_own[0, 1:2, :] = ffn_gain_part
    gain_own[0, 2:8, :] = jnp.zeros((6, width), jnp.float32)

    def gain_send(stage, where):
        return remote(
            gain_own.at[stage], gain_in.at[stage], g_send.at[stage], g_recv.at[stage], where
        )

    gain_hops = [gain_send(0, to_y), gain_send(1, to_c), gain_send(2, to_x)]
    gain_last = [
        remote(
            gain_own.at[3], gain_in.at[2 + step], g_send.at[2 + step], g_recv.at[2 + step], to_z(step)
        )
        for step in range(1, z_size)
    ]

    def gain_fold(stage):
        gain_hops[stage].wait_recv()
        gain_own[stage + 1] = gain_own[stage] + gain_in[stage]

    gain_hops[0].start()
    mix_step(0)
    w_z_stage(0, 0)
    gain_fold(0)
    gain_hops[1].start()
    w_z_stage(1, 2)
    gain_fold(1)
    gain_hops[2].start()
    gain_fold(2)
    for copy in gain_last:
        copy.start()

    kv_over_x.wait_recv()

    def kv_add_x(index, carry):
        block = kv_part.at[index, me_x, me_c, me_y]
        block[...] = (
            block[...].astype(jnp.float32) + kv_x[index].astype(jnp.float32)
        ).astype(jnp.bfloat16)
        return carry

    lax.fori_loop(0, z_size, kv_add_x, 0)
    kv_over_z = [
        remote(
            kv_part.at[lax.rem(me_z + step, z_size), me_x, me_c, me_y],
            kv_z.at[step],
            kz_send.at[step],
            kz_recv.at[step],
            to_z(step),
        )
        for step in range(1, z_size)
    ]
    for copy in kv_over_z:
        copy.start()
    w_z_stage(1, 3)
    for copy in gain_last:
        copy.wait_recv()
    gsum_ref[...] = gain_own[3] + gain_in[3] + gain_in[4] + gain_in[5]
    for copy in kv_over_z:
        copy.wait_recv()
    kvg_ref[...] = (
        kv_part[me_z, me_x, me_c, me_y].astype(jnp.float32)
        + kv_z[1].astype(jnp.float32)
        + kv_z[2].astype(jnp.float32)
        + kv_z[3].astype(jnp.float32)
    )
    w_z_stage(1, 0)

    back_out.wait_send()
    kv_over_y.wait_send()
    kv_over_c.wait_send()
    kv_over_x.wait_send()
    for copy in own_out:
        copy.wait()
    for index in range(len(tasks)):
        f_x(index).wait_send()
    for step in range(1, z_size):
        for kind in range(3):
            f_z(step, kind).wait()
    for copy in gain_hops + gain_last + kv_over_z:
        copy.wait_send()
    for step in range(z_size):
        mix_over_y(step).wait_send()
        if step:
            mix_over_z(step).wait_send()
        for kind in range(2):
            w_c(kind, step, 0).wait_send()
            w_c(kind, step, 1).wait_send()
            w_x(kind, step).wait_send()
            if step:
                w_z(kind, step).wait_send()


def post_call(
    grad_normed,
    mid,
    tokens,
    cotangent,
    gains,
    normed_one,
    rotated,
    keys,
    values,
    attn_vals,
    table,
    allowed,
    kv_weight,
    query_weight,
    out_weight,
    mix_parts,
    ffn_sums,
):
    z_size = lax.axis_size("z")
    own, width = tokens.shape
    seq = 2 * own
    head = keys.shape[1]
    cols = attn_vals.shape[1]
    rows = width // (4 * z_size)
    units = ffn_sums.shape[4]
    low = lambda *dims: pltpu.VMEM(dims, jnp.bfloat16)
    full = lambda *dims: pltpu.VMEM(dims, jnp.float32)
    out_full = lambda *dims: jax.ShapeDtypeStruct(dims, jnp.float32)
    out_low = lambda *dims: jax.ShapeDtypeStruct(dims, jnp.bfloat16)
    dma = lambda *lead: pltpu.SemaphoreType.DMA(lead)
    vmem = pl.BlockSpec(memory_space=pltpu.VMEM)
    hbm = pl.BlockSpec(memory_space=pl.ANY)
    z = z_size
    return pl.pallas_call(
        functools.partial(post_kernel, z_size),
        out_shape=(
            out_low(own, width),
            out_low(own, width),
            out_full(8, width),
            out_full(rows // 2, 2 * head),
            out_full(rows, cols),
            out_full(rows, cols),
            out_low(3, z, rows, units),
        ),
        in_specs=[vmem] * 11 + [hbm] * 6,
        out_specs=(vmem,) * 6 + (hbm,),
        scratch_shapes=[
            low(z, 2, 2, 2, rows // 2, 2 * head),
            low(width, cols),
            low(width, cols),
            low(width, cols),
            low(seq, width),
            full(own, width),
            low(seq, cols),
            low(seq, 2 * head),
            full(2, seq, head),
            low(own, width),
            low(z, own, width),
            low(z - 1, own, width),
            low(z, own, width),
            low(z, 2, rows, cols),
            low(z, rows, cols),
            low(z - 1, rows, cols),
            low(z, 2, rows, cols),
            low(z, rows, cols),
            low(z - 1, rows, cols),
            low(z, 2, 2, rows // 2, 2 * head),
            low(z, 2, rows // 2, 2 * head),
            low(z, rows // 2, 2 * head),
            low(z, rows // 2, 2 * head),
            full(4, 8, width),
            full(6, 8, width),
            low(9, rows, units),
            low(2, rows, units),
            dma(4 + z),
            dma(2),
            dma(3),
            dma(9),
            dma(9),
            dma(3, z),
            dma(3, z),
            dma(3),
            dma(3),
            dma(z),
            dma(z),
            dma(z),
            dma(z),
            dma(2, z, 2),
            dma(2, z, 2),
            dma(2, z),
            dma(2, z),
            dma(2, z),
            dma(2, z),
            dma(2),
            dma(2),
            dma(z),
            dma(z),
            dma(6),
            dma(6),
        ],
        compiler_params=pltpu.CompilerParams(
            collective_id=2, has_side_effects=True, vmem_limit_bytes=VMEM_BYTES
        ),
        cost_estimate=pl.CostEstimate(
            flops=14 * seq * width * cols,
            bytes_accessed=10 * width * cols,
            transcendentals=seq * seq * cols // head,
        ),
    )(
        mid,
        tokens,
        cotangent,
        gains,
        normed_one,
        rotated,
        keys,
        values,
        attn_vals,
        table,
        allowed,
        kv_weight.reshape(z, 2, 2, 2, rows // 2, kv_weight.shape[1]),
        query_weight,
        out_weight,
        mix_parts,
        grad_normed,
        ffn_sums,
    )


def layout_kernel(
    z_size, main, ffn_ref, q_ref, o_ref, kv_ref, wg_ref, wu_ref, wd_ref, qg_ref, og_ref, kvg_ref
):
    me_z = lax.axis_index("z")
    for kind, out in enumerate((wg_ref, wu_ref, wd_ref)):
        out[:, z_size * main :] = jnp.zeros((out.shape[0], 64 * z_size), jnp.float32)
        for step in range(z_size):
            at = lax.rem(me_z - step + z_size, z_size)
            body = pl.ds(pl.multiple_of(at * main, 128), main)
            out[:, body] = ffn_ref[kind, step, :, :main].astype(jnp.float32)
            tail = pl.ds(pl.multiple_of(z_size * main + at // 2 * 128, 128), 128)
            out[:, tail] += ffn_ref[kind, step, :, main:].astype(jnp.float32)
    qg_ref[...] = q_ref[...]
    og_ref[...] = o_ref[...]
    kvg_ref[...] = kv_ref[...]


def layout_call(ffn_grads, query_grad, out_grad, kv_grad, ffn_cols):
    z_size = lax.axis_size("z")
    main, units = ragged_split(ffn_cols, z_size)
    rows, cols = query_grad.shape
    parts = rows // 32
    kv_rows = kv_grad.shape[0] // parts
    full = lambda *dims: jax.ShapeDtypeStruct(dims, jnp.float32)
    row = lambda height, width: pl.BlockSpec((height, width), lambda index: (index, 0))
    specs = [row(32, cols), row(32, cols), row(kv_rows, kv_grad.shape[1])]
    return pl.pallas_call(
        functools.partial(layout_kernel, z_size, main),
        grid=(parts,),
        out_shape=(
            *[full(rows, ffn_cols)] * 3,
            full(rows, cols),
            full(rows, cols),
            full(*kv_grad.shape),
        ),
        in_specs=[
            pl.BlockSpec((3, z_size, 32, units), lambda index: (0, 0, index, 0)),
            *specs,
        ],
        out_specs=(*[row(32, ffn_cols)] * 3, *specs),
        compiler_params=pltpu.CompilerParams(vmem_limit_bytes=32 * 1024 * 1024),
    )(ffn_grads, query_grad, out_grad, kv_grad)


FF_SPLIT = 4


def ffn_pass(normed, grad_out, gate_weight, up_weight, down_weight):
    gate = jnp.dot(normed, gate_weight, preferred_element_type=jnp.float32)
    up_proj = jnp.dot(normed, up_weight, preferred_element_type=jnp.float32)
    grad_hidden = jnp.dot(grad_out, down_weight, preferred_element_type=jnp.float32)
    product, pull = jax.vjp(gelu_product, gate, up_proj)
    hidden = product.astype(jnp.bfloat16)
    grad_gate_f, grad_up_f = pull(grad_hidden)
    grad_gate = grad_gate_f.astype(jnp.bfloat16)
    grad_up = grad_up_f.astype(jnp.bfloat16)
    mixed_part = matmul_nt(hidden, down_weight).astype(jnp.bfloat16)
    normed_part = (matmul_nt(grad_gate, gate_weight) + matmul_nt(grad_up, up_weight)).astype(
        jnp.bfloat16
    )
    weight_parts = [
        matmul_tn(normed, grad_gate).astype(jnp.bfloat16),
        matmul_tn(normed, grad_up).astype(jnp.bfloat16),
        matmul_tn(grad_out, hidden).astype(jnp.bfloat16),
    ]
    return mixed_part, normed_part, weight_parts


def shards_general(
    tokens,
    segments,
    positions,
    cotangent,
    attn_gain,
    ffn_gain,
    w_kv,
    w_query,
    w_out,
    w_gate,
    w_up,
    w_down,
):
    everywhere = ("z", "xc", "mp")
    dp = ("z", "xc")
    z_size = lax.axis_size("z")
    xc_size = lax.axis_size("xc")
    gains = lax.all_gather(
        jnp.stack([attn_gain, ffn_gain], axis=1), everywhere, axis=0, tiled=True
    ).astype(jnp.float32)
    gain_one, gain_two = gains[:, 0], gains[:, 1]
    kv_weight = lax.all_gather(w_kv, everywhere, axis=0, tiled=True)
    head_dim = kv_weight.shape[1] // 2
    width = tokens.shape[1]
    seq_len = segments.shape[0]
    heads_here = w_query.shape[1] // head_dim
    scale = head_dim ** (-0.5)
    cosine, sine = rotary_angles(positions, head_dim)
    inputs_f = tokens.astype(jnp.float32)
    tokens_all = lax.all_gather(tokens, "mp", axis=0, tiled=True)
    normed_one = norm_gain(tokens_all.astype(jnp.float32), gain_one).astype(jnp.bfloat16)
    query_weight = lax.all_gather(w_query, dp, axis=0, tiled=True)
    out_weight = lax.all_gather(w_out, dp, axis=0, tiled=True)

    rows = w_gate.shape[0]
    unit = w_gate.shape[1] // z_size

    def spread(weight):
        pieces = weight.reshape(rows, z_size, unit).transpose(1, 0, 2)
        pieces = lax.all_to_all(pieces, "z", split_axis=0, concat_axis=0, tiled=True)
        return lax.all_gather(pieces, "xc", axis=1, tiled=False).reshape(width, unit)

    gate_weight, up_weight, down_weight = spread(w_gate), spread(w_up), spread(w_down)
    grad_all = lax.all_gather(cotangent, ("z", "mp"), axis=0, tiled=True)

    query = jnp.dot(normed_one, query_weight, preferred_element_type=jnp.float32).reshape(
        seq_len, heads_here, head_dim
    )
    rotated = (rotate(query, cosine[:, None], sine[:, None]) * scale).astype(jnp.bfloat16)
    keyval = jnp.dot(normed_one, kv_weight, preferred_element_type=jnp.float32)
    keys = rotate(keyval[:, :head_dim], cosine, sine).astype(jnp.bfloat16)
    values = keyval[:, head_dim:].astype(jnp.bfloat16)
    allowed = block_allowed(segments, 0, seq_len)
    scores = jnp.einsum("thd,sd->hts", rotated, keys, preferred_element_type=jnp.float32)
    scores = jnp.where(allowed[None], scores, masked_score)
    row_max = jnp.max(scores, axis=-1, keepdims=True)
    weights = jnp.exp(scores - row_max)
    probs = weights / jnp.sum(weights, axis=-1, keepdims=True)
    probs_low = probs.astype(jnp.bfloat16)
    attn_vals = (
        jnp.einsum("hts,sd->thd", probs_low, values, preferred_element_type=jnp.float32)
        .reshape(seq_len, heads_here * head_dim)
        .astype(jnp.bfloat16)
    )
    mid = inputs_f + lax.psum_scatter(
        matmul_nt(attn_vals, out_weight).astype(jnp.bfloat16),
        "mp",
        scatter_dimension=0,
        tiled=True,
    ).astype(jnp.float32)
    normed_two = norm_gain(mid, gain_two).astype(jnp.bfloat16)
    normed_all = lax.all_gather(normed_two, ("z", "mp"), axis=0, tiled=True)

    mixed_part, normed_part, weight_parts = ffn_pass(
        normed_all, grad_all, gate_weight, up_weight, down_weight
    )
    grad_normed_two = lax.psum_scatter(
        normed_part, ("z", "mp"), scatter_dimension=0, tiled=True
    ).astype(jnp.float32)
    mixed = (
        mid
        + lax.psum_scatter(mixed_part, ("z", "mp"), scatter_dimension=0, tiled=True).astype(
            jnp.float32
        )
    ).astype(jnp.bfloat16)

    def collect(part):
        pieces = part.reshape(z_size, xc_size, rows, unit).transpose(1, 0, 2, 3)
        pieces = pieces.reshape(xc_size * z_size * rows, unit)
        pieces = lax.psum_scatter(pieces, "xc", scatter_dimension=0, tiled=True)
        pieces = pieces.reshape(z_size, rows, unit)
        pieces = lax.all_to_all(pieces, "z", split_axis=0, concat_axis=0, tiled=True)
        return pieces.transpose(1, 0, 2).reshape(rows, z_size * unit).astype(jnp.float32)

    w_gate_grad, w_up_grad, w_down_grad = [collect(part) for part in weight_parts]

    norm_pull_two = jax.vjp(norm_gain, mid, gain_two)[1]
    grad_mid_norm, grad_gain_two = norm_pull_two(grad_normed_two)
    grad_mid = cotangent.astype(jnp.float32) + grad_mid_norm
    grad_mid_all = lax.all_gather(grad_mid.astype(jnp.bfloat16), "mp", axis=0, tiled=True)
    grad_vals = (
        jnp.dot(grad_mid_all, out_weight, preferred_element_type=jnp.float32)
        .astype(jnp.bfloat16)
        .reshape(seq_len, heads_here, head_dim)
    )
    grad_probs = jnp.einsum("thd,sd->hts", grad_vals, values, preferred_element_type=jnp.float32)
    delta = jnp.sum(probs * grad_probs, axis=-1, keepdims=True)
    grad_scores = (probs * (grad_probs - delta)).astype(jnp.bfloat16)
    grad_rot = jnp.einsum("hts,sd->thd", grad_scores, keys, preferred_element_type=jnp.float32)
    key_sum = jnp.einsum("hts,thd->sd", grad_scores, rotated, preferred_element_type=jnp.float32)
    value_sum = jnp.einsum("hts,thd->sd", probs_low, grad_vals, preferred_element_type=jnp.float32)
    grad_query = (
        (unrotate(grad_rot, cosine[:, None], sine[:, None]) * scale)
        .reshape(seq_len, heads_here * head_dim)
        .astype(jnp.bfloat16)
    )
    grad_kv = jnp.concatenate([unrotate(key_sum, cosine, sine), value_sum], axis=1).astype(
        jnp.bfloat16
    )
    grad_normed_one = lax.psum_scatter(
        (matmul_nt(grad_query, query_weight) + matmul_nt(grad_kv, kv_weight)).astype(jnp.bfloat16),
        "mp",
        scatter_dimension=0,
        tiled=True,
    ).astype(jnp.float32)
    norm_pull_one = jax.vjp(norm_gain, inputs_f, gain_one)[1]
    grad_input_norm, grad_gain_one = norm_pull_one(grad_normed_one)
    tokens_grad = (grad_mid + grad_input_norm).astype(jnp.bfloat16)

    w_query_grad = lax.psum_scatter(
        matmul_tn(normed_one, grad_query).astype(jnp.bfloat16), dp, scatter_dimension=0, tiled=True
    ).astype(jnp.float32)
    w_out_grad = lax.psum_scatter(
        matmul_tn(grad_mid_all, attn_vals).astype(jnp.bfloat16), dp, scatter_dimension=0, tiled=True
    ).astype(jnp.float32)
    small = jnp.concatenate(
        [matmul_tn(normed_one, grad_kv), grad_gain_one[:, None], grad_gain_two[:, None]], axis=1
    )
    small = lax.psum_scatter(small, everywhere, scatter_dimension=0, tiled=True)
    kv_grad = small[:, : 2 * head_dim]
    return (
        mixed,
        tokens_grad,
        small[:, 2 * head_dim],
        small[:, 2 * head_dim + 1],
        kv_grad,
        w_query_grad,
        w_out_grad,
        w_gate_grad,
        w_up_grad,
        w_down_grad,
    )


def shards_fast(
    tokens,
    segments,
    positions,
    cotangent,
    attn_gain,
    ffn_gain,
    w_kv,
    w_query,
    w_out,
    w_gate,
    w_up,
    w_down,
):
    seq_len = segments.shape[0]
    cosine, sine = rotary_angles(positions, w_kv.shape[1] // 2)
    table = jnp.stack(
        [
            jnp.concatenate([cosine, cosine], axis=1),
            jnp.concatenate([-sine, sine], axis=1),
        ]
    )
    allowed = block_allowed(segments, 0, seq_len).astype(jnp.float32)
    kv_gains = jnp.concatenate(
        [w_kv, attn_gain[:, None], ffn_gain[:, None], jnp.zeros((w_kv.shape[0], 126), w_kv.dtype)],
        axis=1,
    )
    (
        normed_one,
        rotated,
        keys,
        values,
        attn_vals,
        mid,
        normed_two,
        gains,
        kv_weight,
        query_weight,
        out_weight,
        ffn_weights,
        grad_all,
    ) = pre_call(
        tokens, kv_gains, table, allowed, cotangent, w_query, w_out, (w_gate, w_up, w_down)
    )
    main = ragged_split(w_gate.shape[1], lax.axis_size("z"))[0]
    grad_normed_two, mix_parts, ffn_sums = ffn_call(
        normed_two, grad_all, ffn_weights, w_gate.shape[0], main
    )
    mixed, tokens_grad, gain_grads, kv_grad, query_grad, out_grad, ffn_grads = post_call(
        grad_normed_two,
        mid,
        tokens,
        cotangent,
        gains,
        normed_one,
        rotated,
        keys,
        values,
        attn_vals,
        table,
        allowed,
        kv_weight,
        query_weight,
        out_weight,
        mix_parts,
        ffn_sums,
    )
    *ffn_out, query_grad, out_grad, kv_grad = layout_call(
        ffn_grads, query_grad, out_grad, kv_grad, w_gate.shape[1]
    )
    share = attn_gain.shape[0]
    place = lax.axis_index(("z", "x", "c", "mp")) * share
    gain_grads = lax.dynamic_slice(gain_grads, (0, place), (2, share))
    return (
        mixed,
        tokens_grad,
        gain_grads[0],
        gain_grads[1],
        kv_grad,
        query_grad,
        out_grad,
        *ffn_out,
    )


def solution(mesh):
    dp_size, mp_size = mesh.shape["dp"], mesh.shape["mp"]
    if dp_size == 4 * FF_SPLIT and mp_size == 2:
        body, dp = shards_fast, ("z", "x", "c")
        sizes = (FF_SPLIT, 2, 2, mp_size)
    else:
        body, dp = shards_general, ("z", "xc")
        sizes = (FF_SPLIT, dp_size // FF_SPLIT, mp_size)
    all_axes = (*dp, "mp")
    fine = jax.sharding.Mesh(mesh.devices.reshape(sizes), all_axes)
    in_specs = (
        P(all_axes, None),
        P(dp),
        P(dp),
        P(all_axes, None),
        P(all_axes),
        P(all_axes),
        P(all_axes, None),
        P(dp, "mp"),
        P(dp, "mp"),
        P(dp, "mp"),
        P(dp, "mp"),
        P(dp, "mp"),
    )
    out_specs = (
        P(all_axes, None),
        P(all_axes, None),
        P(all_axes),
        P(all_axes),
        P(all_axes, None),
        P(dp, "mp"),
        P(dp, "mp"),
        P(dp, "mp"),
        P(dp, "mp"),
        P(dp, "mp"),
    )
    return jax.shard_map(body, mesh=fine, in_specs=in_specs, out_specs=out_specs, check_vma=False)
```

```python
import functools

import jax
import jax.numpy as jnp
from jax import lax
from jax.experimental import pallas as pl
from jax.experimental.pallas import tpu as pltpu
from jax.sharding import PartitionSpec as P

WINDOW = 2048


epsilon = 1e-06
rope_base = 10000.0
masked_score = -1e30
VMEM_BYTES = 66_000_000


def norm_gain(values, gain):
    return values * lax.rsqrt(jnp.mean(values * values, axis=-1, keepdims=True) + epsilon) * gain


def rotary_angles(positions, head_width):
    quarter = head_width // 4
    freqs = rope_base ** (-jnp.arange(quarter).astype(jnp.float32) / quarter)
    phase = positions.astype(jnp.float32)[:, None] * freqs[None, :]
    return (jnp.cos(phase), jnp.sin(phase))


def rotate(values, cosine, sine):
    quarter = cosine.shape[-1]
    first_half = values[..., :quarter]
    second_half = values[..., quarter : 2 * quarter]
    return jnp.concatenate(
        [
            first_half * cosine - second_half * sine,
            second_half * cosine + first_half * sine,
            values[..., 2 * quarter :],
        ],
        axis=-1,
    )


def unrotate(values, cosine, sine):
    quarter = cosine.shape[-1]
    first_half = values[..., :quarter]
    second_half = values[..., quarter : 2 * quarter]
    return jnp.concatenate(
        [
            first_half * cosine + second_half * sine,
            second_half * cosine - first_half * sine,
            values[..., 2 * quarter :],
        ],
        axis=-1,
    )


def gelu_product(gate, up_proj):
    return jax.nn.gelu(gate, approximate=True) * up_proj


def matmul_nt(left, right):
    return lax.dot_general(
        left, right, (((1,), (1,)), ((), ())), preferred_element_type=jnp.float32
    )


def matmul_tn(left, right):
    return lax.dot_general(
        left, right, (((0,), (0,)), ((), ())), preferred_element_type=jnp.float32
    )


def block_allowed(segments, first_row, rows):
    seq_len = segments.shape[0]
    query_rows = first_row + jnp.arange(rows)
    key_rows = jnp.arange(seq_len)
    return (
        (segments[:, None] == segments[None, :])
        & (key_rows[None, :] <= query_rows[:, None])
        & (query_rows[:, None] - key_rows[None, :] < WINDOW)
    )


MESH_ID = pl.DeviceIdType.MESH
GELU_A = 0.7978845608028654
GELU_B = 0.044715
TILE = 256
WIDE = 512


def remote(src, dst, send_sem, recv_sem, where):
    return pltpu.make_async_remote_copy(
        src_ref=src,
        dst_ref=dst,
        send_sem=send_sem,
        recv_sem=recv_sem,
        device_id=where,
        device_id_type=MESH_ID,
    )


def dot_nn(left, right):
    return lax.dot_general(
        left, right, (((1,), (0,)), ((), ())), preferred_element_type=jnp.float32
    )


def gelu_parts(gate):
    square = gate * gate
    bend = jnp.tanh(GELU_A * gate * (1.0 + GELU_B * square))
    half = 0.5 * (1.0 + bend)
    slope = half + 0.5 * gate * (1.0 - bend * bend) * GELU_A * (1.0 + 3.0 * GELU_B * square)
    return gate * half, slope


def add_rows(first, rest, out, count):
    def body(index, carry):
        step = pl.ds(pl.multiple_of(index * 32, 32), 32)
        total = first[step, :].astype(jnp.float32)
        for other in rest:
            total = total + other[step, :].astype(jnp.float32)
        out[step, :] = total.astype(out.dtype)
        return carry

    lax.fori_loop(0, count // 32, body, 0)


def ffn_kernel(
    z_size,
    main,
    own_ref,
    dy_hbm,
    w_hbm,
    gn_ref,
    mix_hbm,
    sums_hbm,
    n2,
    dy,
    w3,
    h3,
    left_t,
    gn_part,
    mix_buf,
    gn_y,
    gn_z,
    gn_s,
    c_in,
    x_in,
    load_sem,
    mix_sem,
    ag_y_send,
    ag_y_recv,
    ag_z_send,
    ag_z_recv,
    rs_y_send,
    rs_y_recv,
    rs_z_send,
    rs_z_recv,
    c_send,
    c_recv,
    x_send,
    x_recv,
    out_sem,
):
    own = own_ref.shape[0] // 2
    width = own_ref.shape[1]
    units = w3.shape[2]
    rows = c_in.shape[3]
    span = width // z_size
    me_y, me_z = lax.axis_index("mp"), lax.axis_index("z")
    me_x, me_c = lax.axis_index("x"), lax.axis_index("c")
    mine = pl.ds(pl.multiple_of(me_y * own, own), own)
    theirs = pl.ds(pl.multiple_of((1 - me_y) * own, own), own)
    to_y, to_x, to_c = {"mp": 1 - me_y}, {"x": 1 - me_x}, {"c": 1 - me_c}

    def ahead(step):
        return lax.rem(me_z + step, z_size)

    def to_z(step):
        return {"z": ahead(step)}

    def row_block(z_at, x_at, c_at):
        return pl.ds(pl.multiple_of(((z_at * 2 + x_at) * 2 + c_at) * rows, rows), rows)

    loads = []
    for index in range(z_size):
        loads.append(pltpu.make_async_copy(dy_hbm.at[index], dy.at[index], load_sem.at[index]))
    for index in range(3):
        loads.append(
            pltpu.make_async_copy(w_hbm.at[index], w3.at[index], load_sem.at[z_size + index])
        )
    for load in loads:
        load.start()

    barrier = pltpu.get_barrier_semaphore()
    peers = [to_y, to_x, to_c] + [to_z(step) for step in range(1, z_size)]
    for where in peers:
        pl.semaphore_signal(barrier, inc=1, device_id=where, device_id_type=MESH_ID)
    pl.semaphore_wait(barrier, len(peers))

    def ag_y(index):
        block = n2.at[index, mine]
        return remote(block, block, ag_y_send.at[index], ag_y_recv.at[index], to_y)

    def ag_y_in(index):
        block = n2.at[index, theirs]
        return remote(block, block, ag_y_send.at[index], ag_y_recv.at[index], to_y)

    def ag_z(index):
        src = own_ref.at[mine] if index == 0 else n2.at[index, mine]
        return remote(
            src, n2.at[index + 1, mine], ag_z_send.at[index], ag_z_recv.at[index + 1], to_z(1)
        )

    def ag_z_in(index):
        block = n2.at[index, mine]
        return remote(block, block, ag_z_send.at[0], ag_z_recv.at[index], to_z(1))

    def forward(index):
        ag_z_in(index).wait_recv()
        if index < z_size - 1:
            ag_z(index).start()
        ag_y(index).start()

    ag_z(0).start()
    n2[0] = own_ref[...]

    mix_copies = []

    def chunk(index):
        if index:
            ag_y_in(index).wait_recv()
        if index >= 2:
            mix_copies[index - 2].wait()
        rows_at = pl.ds(index * 2 * own, 2 * own)

        def up_tile(tile, carry):
            cols = pl.ds(pl.multiple_of(tile * WIDE, WIDE), WIDE)
            normed = n2[index]
            gate = dot_nn(normed, w3[0, :, cols])
            up_proj = dot_nn(normed, w3[1, :, cols])
            grad_hidden = dot_nn(dy[index], w3[2, :, cols])
            act, slope = gelu_parts(gate)
            at = lax.broadcasted_iota(jnp.int32, (1, WIDE), 1) + tile * WIDE
            low_at = main + 64 * lax.rem(me_z, 2)
            keep = (at < main) | ((at >= low_at) & (at < low_at + 64))
            act = jnp.where(keep, act, 0.0)
            slope = jnp.where(keep, slope, 0.0)
            h3[0, rows_at, cols] = (grad_hidden * up_proj * slope).astype(jnp.bfloat16)
            h3[1, rows_at, cols] = (grad_hidden * act).astype(jnp.bfloat16)
            h3[2, rows_at, cols] = (act * up_proj).astype(jnp.bfloat16)
            return carry

        lax.fori_loop(0, units // WIDE, up_tile, 0)

        def down_tile(tile, carry):
            cols = pl.ds(pl.multiple_of(tile * span, 128), span)
            gn_part[index, :, cols] = (
                matmul_nt(h3[0, rows_at, :], w3[0, cols, :])
                + matmul_nt(h3[1, rows_at, :], w3[1, cols, :])
            ).astype(jnp.bfloat16)
            mix_buf[index % 2, :, cols] = matmul_nt(h3[2, rows_at, :], w3[2, cols, :]).astype(
                jnp.bfloat16
            )
            return carry

        lax.fori_loop(0, z_size, down_tile, 0)
        copy = pltpu.make_async_copy(mix_buf.at[index % 2], mix_hbm.at[index], mix_sem.at[index])
        copy.start()
        mix_copies.append(copy)

    def rs_y(index):
        return remote(
            gn_part.at[index, theirs], gn_y.at[index], rs_y_send.at[index], rs_y_recv.at[index], to_y
        )

    def rs_z(index):
        return remote(
            gn_s.at[index - 1],
            gn_z.at[index - 1],
            rs_z_send.at[index],
            rs_z_recv.at[index - 1],
            to_z(1),
        )

    def rs_step(index):
        rs_y(index).wait_recv()
        slot = (index - 2) % z_size
        if index != 1:
            remote(
                gn_s.at[slot], gn_z.at[slot], rs_z_send.at[1], rs_z_recv.at[slot], to_z(1)
            ).wait_recv()

        def add_tile(tile, carry):
            cols = pl.ds(pl.multiple_of(tile * TILE, TILE), TILE)
            total = gn_part[index, mine, cols].astype(jnp.float32) + gn_y[index, :, cols].astype(
                jnp.float32
            )
            if index != 1:
                total = total + gn_z[slot, :, cols].astype(jnp.float32)
            if index == 0:
                gn_ref[:, cols] = total
            else:
                gn_s[index - 1, :, cols] = total.astype(jnp.bfloat16)
            return carry

        lax.fori_loop(0, width // TILE, add_tile, 0)
        if index != 0:
            rs_z(index).start()


    def grads(step):
        at = pl.ds(pl.multiple_of(ahead(step) * span, 128), span)
        for kinds, source in (((0, 1), n2), ((2,), dy)):
            left_t[...] = source[:, :, at].reshape(z_size * 2 * own, span).T
            for kind in kinds:

                def tile_body(tile, carry, kind=kind):
                    cols = pl.ds(pl.multiple_of(tile * WIDE, WIDE), WIDE)
                    w3[kind, at, cols] = dot_nn(left_t[...], h3[kind, :, cols]).astype(jnp.bfloat16)
                    return carry

                lax.fori_loop(0, units // WIDE, tile_body, 0)
        for far in (1, 0):
            for kind in range(3):
                over_c(kind, step, far).start()

    def over_c(kind, step, far):
        x_at = 1 - me_x if far else me_x
        return remote(
            w3.at[kind, row_block(ahead(step), x_at, 1 - me_c)],
            c_in.at[kind, step, far],
            c_send.at[kind, step, far],
            c_recv.at[kind, step, far],
            to_c,
        )

    def over_x(kind):
        return remote(
            w3.at[kind, row_block(ahead(1), 1 - me_x, me_c)],
            x_in.at[kind],
            x_send.at[kind],
            x_recv.at[kind],
            to_x,
        )

    out_copies = []

    def keep(kind, step, far, block):
        copy = pltpu.make_async_copy(
            block, sums_hbm.at[kind, step, far], out_sem.at[kind, step, far]
        )
        copy.start()
        out_copies.append(copy)

    def core_sums(step):
        for far in (1, 0):
            for kind in range(3):
                over_c(kind, step, far).wait_recv()
                x_at = 1 - me_x if far else me_x
                block = w3.at[kind, row_block(ahead(step), x_at, me_c)]
                add_rows(block, [c_in.at[kind, step, far]], block, rows)
                if step != 1:
                    keep(kind, step, far, block)
                elif far:
                    over_x(kind).start()

    def first_sums():
        for kind in range(3):
            over_x(kind).wait_recv()
            block = w3.at[kind, row_block(ahead(1), me_x, me_c)]
            add_rows(block, [x_in.at[kind]], block, rows)
            keep(kind, 1, 0, block)

    forward(1)
    for load in loads:
        load.wait()
    chunk(0)
    rs_y(0).start()
    forward(2)
    chunk(1)
    rs_y(1).start()
    forward(3)
    chunk(2)
    rs_y(2).start()
    rs_step(1)
    chunk(3)
    rs_y(3).start()
    rs_step(2)
    grads(1)
    grads(2)
    core_sums(1)
    rs_step(3)
    grads(3)
    core_sums(2)
    grads(0)
    core_sums(3)
    rs_step(0)
    core_sums(0)
    first_sums()

    for copy in mix_copies[2:] + out_copies:
        copy.wait()
    for index in range(z_size):
        if index:
            ag_y(index).wait_send()
        rs_y(index).wait_send()
        if index < z_size - 1:
            ag_z(index).wait_send()
        if index:
            rs_z(index).wait_send()
        for kind in range(3):
            over_c(kind, index, 0).wait_send()
            over_c(kind, index, 1).wait_send()
            if index == 1:
                over_x(kind).wait_send()


def ffn_call(normed, grad_all, weights, rows, main):
    z_size = lax.axis_size("z")
    pair, width = normed.shape
    units = weights.shape[2]
    own = pair // 2
    wide = lambda *lead: pltpu.VMEM((*lead, width), jnp.bfloat16)
    dma = lambda *lead: pltpu.SemaphoreType.DMA(lead)
    vmem = pl.BlockSpec(memory_space=pltpu.VMEM)
    hbm = pl.BlockSpec(memory_space=pl.ANY)
    return pl.pallas_call(
        functools.partial(ffn_kernel, z_size, main),
        out_shape=(
            jax.ShapeDtypeStruct((own, width), jnp.float32),
            jax.ShapeDtypeStruct((z_size, pair, width), jnp.bfloat16),
            jax.ShapeDtypeStruct((3, z_size, 2, rows, units), jnp.bfloat16),
        ),
        in_specs=[vmem, hbm, hbm],
        out_specs=(vmem, hbm, hbm),
        scratch_shapes=[
            wide(z_size, pair),
            wide(z_size, pair),
            pltpu.VMEM(weights.shape, jnp.bfloat16),
            pltpu.VMEM((3, z_size * pair, units), jnp.bfloat16),
            pltpu.VMEM((width // z_size, z_size * pair), jnp.bfloat16),
            wide(z_size, pair),
            wide(2, pair),
            wide(z_size, own),
            wide(z_size - 1, own),
            wide(z_size - 1, own),
            pltpu.VMEM((3, z_size, 2, rows, units), jnp.bfloat16),
            pltpu.VMEM((3, rows, units), jnp.bfloat16),
            dma(z_size + 3),
            dma(z_size),
            dma(z_size),
            dma(z_size),
            dma(z_size),
            dma(z_size),
            dma(z_size),
            dma(z_size),
            dma(z_size),
            dma(z_size),
            dma(3, z_size, 2),
            dma(3, z_size, 2),
            dma(3),
            dma(3),
            dma(3, z_size, 2),
        ],
        compiler_params=pltpu.CompilerParams(
            collective_id=0, has_side_effects=True, vmem_limit_bytes=VMEM_BYTES
        ),
        cost_estimate=pl.CostEstimate(
            flops=18 * z_size * pair * width * units,
            bytes_accessed=4 * weights.size + 12 * z_size * pair * width,
            transcendentals=z_size * pair * units,
        ),
    )(normed, grad_all, weights)


def spin(values, table):
    first = values[:, : values.shape[1] // 2]
    turned = first * table[0] + pltpu.roll(first, first.shape[1] // 2, 1) * table[1]
    return jnp.concatenate([turned, values[:, values.shape[1] // 2 :]], axis=1)


def spin_back(values, table):
    first = values[:, : values.shape[1] // 2]
    turned = first * table[0] - pltpu.roll(first, first.shape[1] // 2, 1) * table[1]
    return jnp.concatenate([turned, values[:, values.shape[1] // 2 :]], axis=1)


def head_probs(rotated, keys, allowed):
    scores = jnp.where(allowed > 0.5, matmul_nt(rotated, keys), masked_score)
    weights = jnp.exp(scores - jnp.max(scores, axis=-1, keepdims=True))
    return weights / jnp.sum(weights, axis=-1, keepdims=True)


def ragged_split(columns, parts):
    main = columns // parts // 128 * 128
    return main, main + 128


def pre_kernel(
    z_size,
    tok_ref,
    kvg_ref,
    table_ref,
    allow_ref,
    cot_hbm,
    wq_hbm,
    wo_hbm,
    wg_hbm,
    wu_hbm,
    wd_hbm,
    n1_ref,
    rot_ref,
    key_ref,
    val_ref,
    att_ref,
    mid_ref,
    n2_ref,
    gain_ref,
    kv_out,
    wq_out,
    wo_out,
    w3_out,
    dy_out,
    kv_w,
    q_w,
    o_w,
    tok,
    part,
    part_y,
    query,
    y_send,
    y_recv,
    az_send,
    az_recv,
    ax_send,
    ax_recv,
    ac_send,
    ac_recv,
    fz_send,
    fz_recv,
    fx_send,
    fx_recv,
    fc_send,
    fc_recv,
    dz_send,
    dz_recv,
    dy_send,
    dy_recv,
    local_sem,
):
    me_z, me_x = lax.axis_index("z"), lax.axis_index("x")
    me_c, me_y = lax.axis_index("c"), lax.axis_index("mp")
    own, width = tok_ref.shape
    rows = wq_hbm.shape[0]
    half_rows = kvg_ref.shape[0]
    head = key_ref.shape[1]
    main, units = ragged_split(wg_hbm.shape[1], z_size)
    to_y, to_x, to_c = {"mp": 1 - me_y}, {"x": 1 - me_x}, {"c": 1 - me_c}

    def to_z(step):
        return {"z": lax.rem(me_z + step, z_size)}

    def from_z(step):
        return lax.rem(me_z - step + z_size, z_size)

    def row_block(step, x_at, c_at):
        start = ((from_z(step) * 2 + x_at) * 2 + c_at) * rows
        return pl.ds(pl.multiple_of(start, rows), rows)

    mine = pl.ds(pl.multiple_of(me_y * own, own), own)
    theirs = pl.ds(pl.multiple_of((1 - me_y) * own, own), own)
    bufs = (kv_w, q_w, o_w)
    inputs = (None, wq_hbm, wo_hbm)

    locals_ = []

    def local(src, dst):
        copy = pltpu.make_async_copy(src, dst, local_sem.at[len(locals_)])
        copy.start()
        locals_.append(copy)
        return copy

    here = row_block(0, me_x, me_c)
    own_q = local(wq_hbm, q_w.at[here])
    own_o = local(wo_hbm, o_w.at[here])
    ffn_in = (wg_hbm, wu_hbm, wd_hbm)

    def pieces(target):
        yield pl.ds(pl.multiple_of(target * main, 128), main), pl.ds(0, main)
        tail = (z_size * main) + (target // 2) * 128
        yield pl.ds(pl.multiple_of(tail, 128), 128), pl.ds(main, 128)

    own_f = []
    for kind in range(3):
        for src, dst in pieces(me_z):
            own_f.append(local(ffn_in[kind].at[:, src], w3_out.at[kind, here, dst]))
    own_d = local(cot_hbm, dy_out.at[0, mine])

    barrier = pltpu.get_barrier_semaphore()
    peers = [to_y, to_x, to_c] + [to_z(step) for step in range(1, z_size)]
    for where in peers:
        pl.semaphore_signal(barrier, inc=1, device_id=where, device_id_type=MESH_ID)
    pl.semaphore_wait(barrier, len(peers))

    kv_mine = pl.ds(pl.multiple_of(here.start + me_y * half_rows, half_rows), half_rows)
    kv_theirs = pl.ds(pl.multiple_of(here.start + (1 - me_y) * half_rows, half_rows), half_rows)
    kv_y = remote(kvg_ref, kv_w.at[kv_mine], y_send.at[0], y_recv.at[0], to_y)
    kv_y_in = remote(kvg_ref, kv_w.at[kv_theirs], y_send.at[0], y_recv.at[0], to_y)
    tok_y = remote(tok_ref, tok.at[mine], y_send.at[1], y_recv.at[1], to_y)
    tok_y_in = remote(tok_ref, tok.at[theirs], y_send.at[1], y_recv.at[1], to_y)
    part_out = remote(part.at[theirs], part_y, y_send.at[2], y_recv.at[2], to_y)
    n2_y = remote(n2_ref.at[mine], n2_ref.at[mine], y_send.at[3], y_recv.at[3], to_y)
    n2_y_in = remote(n2_ref.at[theirs], n2_ref.at[theirs], y_send.at[3], y_recv.at[3], to_y)

    def source(kind, step):
        if isinstance(step, int) and step == 0 and kind:
            return inputs[kind]
        return bufs[kind].at[row_block(step, me_x, me_c)]

    first_z, last_z = (z_size - 1 - me_z) // (z_size - 1), me_z // (z_size - 1)
    inner = first_z + last_z == 0
    order = (0, 1 + 2 * first_z, 3 - first_z - last_z, 2 - first_z + last_z)
    hops = (
        None,
        (lax.rem(me_z + 1, z_size), 2),
        (lax.rem(me_z + z_size - 1, z_size), 2),
        (lax.rem(3 * (me_z + 3), z_size), lax.rem(2 * me_z + 3, z_size)),
    )

    def a_z_own(kind, right):
        return remote(
            source(kind, 0),
            bufs[kind].at[here],
            az_send.at[kind, right],
            az_recv.at[kind, 1 if right else z_size - 1],
            to_z(1 if right else z_size - 1),
        )

    def a_z_start(kind):
        @pl.when(last_z == 0)
        def _():
            a_z_own(kind, 1).start()

        @pl.when(first_z == 0)
        def _():
            a_z_own(kind, 0).start()

    def a_z(kind, index):
        target, slot = hops[index]
        block = bufs[kind].at[row_block(order[index], me_x, me_c)]
        return remote(
            block, block, az_send.at[kind, 1 + index], az_recv.at[kind, slot], {"z": target}
        )

    def a_z_next(kind, index):
        @pl.when(inner)
        def _():
            a_z(kind, index).start()

    def a_z_done(kind):
        @pl.when(last_z == 0)
        def _():
            a_z_own(kind, 1).wait_send()

        @pl.when(first_z == 0)
        def _():
            a_z_own(kind, 0).wait_send()

        @pl.when(inner)
        def _():
            for index in range(1, z_size):
                a_z(kind, index).wait_send()

    def a_z_in(kind, step):
        block = bufs[kind].at[row_block(step, me_x, me_c)]
        return remote(block, block, az_send.at[kind, 0], az_recv.at[kind, step], to_z(1))

    def a_x(kind, step):
        return remote(
            source(kind, step),
            bufs[kind].at[row_block(step, me_x, me_c)],
            ax_send.at[kind, step],
            ax_recv.at[kind, step],
            to_x,
        )

    def a_x_in(kind, step):
        block = bufs[kind].at[row_block(step, 1 - me_x, me_c)]
        return remote(block, block, ax_send.at[kind, step], ax_recv.at[kind, step], to_x)

    def a_c(kind, step, far):
        x_at = 1 - me_x if far else me_x
        block = bufs[kind].at[row_block(step, x_at, me_c)]
        src = block if far else source(kind, step)
        slot = step + z_size * far
        return remote(src, block, ac_send.at[kind, slot], ac_recv.at[kind, slot], to_c)

    def a_c_in(kind, step, far):
        x_at = 1 - me_x if far else me_x
        block = bufs[kind].at[row_block(step, x_at, 1 - me_c)]
        slot = step + z_size * far
        return remote(block, block, ac_send.at[kind, slot], ac_recv.at[kind, slot], to_c)

    def f_z(kind, step):
        target = lax.rem(me_z + step, z_size)
        return [
            remote(
                ffn_in[kind].at[:, src],
                w3_out.at[kind, here, dst],
                fz_send.at[kind, step, index],
                fz_recv.at[kind, step, index],
                to_z(step),
            )
            for index, (src, dst) in enumerate(pieces(target))
        ]

    def f_z_in(kind, step):
        block = row_block(step, me_x, me_c)
        return [
            remote(
                w3_out.at[kind, block, dst],
                w3_out.at[kind, block, dst],
                fz_send.at[kind, step, index],
                fz_recv.at[kind, step, index],
                to_z(step),
            )
            for index, (_, dst) in enumerate(pieces(me_z))
        ]

    def f_x(kind, step):
        block = w3_out.at[kind, row_block(step, me_x, me_c)]
        return remote(block, block, fx_send.at[kind, step], fx_recv.at[kind, step], to_x)

    def f_x_in(kind, step):
        block = w3_out.at[kind, row_block(step, 1 - me_x, me_c)]
        return remote(block, block, fx_send.at[kind, step], fx_recv.at[kind, step], to_x)

    def f_c(kind, step, far):
        block = w3_out.at[kind, row_block(step, 1 - me_x if far else me_x, me_c)]
        slot = step + z_size * far
        return remote(block, block, fc_send.at[kind, slot], fc_recv.at[kind, slot], to_c)

    def f_c_in(kind, step, far):
        block = w3_out.at[kind, row_block(step, 1 - me_x if far else me_x, 1 - me_c)]
        slot = step + z_size * far
        return remote(block, block, fc_send.at[kind, slot], fc_recv.at[kind, slot], to_c)

    def d_source(step):
        return cot_hbm if step == 0 else dy_out.at[step, mine]

    def d_z(step):
        return remote(
            d_source(step), dy_out.at[step + 1, mine], dz_send.at[step], dz_recv.at[step + 1], to_z(1)
        )

    def d_z_in(step):
        block = dy_out.at[step, mine]
        return remote(block, block, dz_send.at[0], dz_recv.at[step], to_z(1))

    def d_y(step):
        return remote(
            d_source(step), dy_out.at[step, mine], dy_send.at[step], dy_recv.at[step], to_y
        )

    def d_y_in(step):
        block = dy_out.at[step, theirs]
        return remote(block, block, dy_send.at[step], dy_recv.at[step], to_y)

    kv_y.start()
    tok_y.start()
    for kind in (1, 2):
        a_z_start(kind)
        a_x(kind, 0).start()
        a_c(kind, 0, 0).start()
    kv_w[kv_mine, :] = kvg_ref[...]
    tok[mine, :] = tok_ref[...]
    kv_y_in.wait_recv()
    a_z_start(0)
    a_x(0, 0).start()
    a_c(0, 0, 0).start()
    d_y(0).start()
    for step in range(1, z_size):
        for kind in (1, 0, 2):
            a_z_in(kind, order[step]).wait_recv()
            a_z_next(kind, step)
            a_x(kind, order[step]).start()
            a_c(kind, order[step], 0).start()
        if step == z_size - 2:
            for copy in own_f:
                copy.wait()
            d_z(0).start()
            for kind in range(3):
                for away in (1, 3, 2):
                    for copy in f_z(kind, away):
                        copy.start()
        for kind in (1, 0, 2):
            a_x_in(kind, order[step - 1]).wait_recv()
            a_c(kind, order[step - 1], 1).start()
    for kind in range(3):
        f_x(kind, 0).start()
        f_c(kind, 0, 0).start()

    def hand_on(kind, step):
        for copy in f_z_in(kind, step):
            copy.wait_recv()
        f_x(kind, step).start()
        f_c(kind, step, 0).start()

    def cross(kind, step):
        f_x_in(kind, step).wait_recv()
        f_c(kind, step, 1).start()

    def pass_cotangent(step):
        d_z_in(step).wait_recv()
        if step < z_size - 1:
            d_z(step).start()
        d_y(step).start()

    pass_cotangent(1)
    for kind in (1, 0, 2):
        a_x_in(kind, order[z_size - 1]).wait_recv()
        a_c(kind, order[z_size - 1], 1).start()
    hand_on(0, 1)
    tok_y_in.wait_recv()
    own_q.wait()
    own_o.wait()
    for kind in (0, 1):
        for step in range(z_size):
            for far in range(2):
                a_c_in(kind, step, far).wait_recv()

    gains = kv_w[:, 2 * head :].astype(jnp.float32).T[:8, :]
    gain_ref[...] = gains

    def norm_rows(index, carry):
        at = pl.ds(pl.multiple_of(index * 32, 32), 32)
        values = tok[at, :].astype(jnp.float32)
        scale = lax.rsqrt(jnp.mean(values * values, axis=-1, keepdims=True) + epsilon)
        n1_ref[at, :] = (values * scale * gain_ref[0:1, :]).astype(jnp.bfloat16)
        return carry

    lax.fori_loop(0, 2 * own // 32, norm_rows, 0)
    hand_on(0, 3)
    table = (table_ref[0], table_ref[1])
    key_ref[...] = spin(dot_nn(n1_ref[...], kv_w[:, :head]), table).astype(jnp.bfloat16)
    val_ref[...] = dot_nn(n1_ref[...], kv_w[:, head : 2 * head]).astype(jnp.bfloat16)
    hand_on(0, 2)
    head_scale = head ** (-0.5)
    heads = att_ref.shape[1] // head

    half_cols = att_ref.shape[1] // 2
    for index in range(2):
        cols = pl.ds(index * half_cols, half_cols)
        query[:, cols] = dot_nn(n1_ref[...], q_w[:, cols])

    def attend(index):
        cols = pl.ds(index * head, head)
        rotated = (spin(query[:, cols], table) * head_scale).astype(jnp.bfloat16)
        rot_ref[:, cols] = rotated
        probs = head_probs(rotated, key_ref[...], allow_ref[...]).astype(jnp.bfloat16)
        att_ref[:, cols] = dot_nn(probs, val_ref[...]).astype(jnp.bfloat16)

    tasks = [
        lambda: cross(0, 0),
        lambda: hand_on(1, 1),
        lambda: pass_cotangent(2),
        lambda: hand_on(1, 3),
        lambda: cross(1, 0),
    ]
    for index in range(heads):
        attend(index)
        if index < len(tasks):
            tasks[index]()
    for step in range(z_size):
        for far in range(2):
            a_c_in(2, step, far).wait_recv()
    saves = [
        local(kv_w, kv_out),
        local(q_w, wq_out),
        local(o_w, wo_out),
    ]
    span = width // 4

    def project(index, carry):
        cols = pl.ds(pl.multiple_of(index * span, span), span)
        part[:, cols] = matmul_nt(att_ref[...], o_w[cols, :]).astype(jnp.bfloat16)
        return carry

    lax.fori_loop(0, 4, project, 0)
    part_out.start()
    hand_on(1, 2)
    cross(2, 0)
    cross(0, 1)
    hand_on(2, 1)
    part_out.wait_recv()

    def middle(index, carry):
        at = pl.ds(pl.multiple_of(index * 32, 32), 32)
        there = pl.ds(pl.multiple_of(me_y * own + index * 32, 32), 32)
        values = (
            tok_ref[at, :].astype(jnp.float32)
            + part[there, :].astype(jnp.float32)
            + part_y[at, :].astype(jnp.float32)
        )
        mid_ref[at, :] = values
        scale = lax.rsqrt(jnp.mean(values * values, axis=-1, keepdims=True) + epsilon)
        n2_ref[there, :] = (values * scale * gain_ref[1:2, :]).astype(jnp.bfloat16)
        return carry

    lax.fori_loop(0, own // 32, middle, 0)
    n2_y.start()
    cross(0, 3)
    hand_on(2, 3)
    pass_cotangent(3)
    cross(0, 2)
    hand_on(2, 2)
    for kind in (1, 2):
        for step in (1, 3, 2):
            cross(kind, step)
    for kind in range(3):
        for step in range(z_size):
            for far in range(2):
                f_c_in(kind, step, far).wait_recv()
    for step in range(z_size):
        d_y_in(step).wait_recv()
    n2_y_in.wait_recv()

    for kind in range(3):
        a_z_done(kind)
    kv_y.wait_send()
    tok_y.wait_send()
    part_out.wait_send()
    n2_y.wait_send()
    own_d.wait()
    for copy in saves:
        copy.wait()
    for step in range(z_size):
        d_y(step).wait_send()
        if step < z_size - 1:
            d_z(step).wait_send()
        for kind in range(3):
            if step:
                for copy in f_z(kind, step):
                    copy.wait_send()
            a_x(kind, step).wait_send()
            f_x(kind, step).wait_send()
            for far in range(2):
                a_c(kind, step, far).wait_send()
                f_c(kind, step, far).wait_send()


def pre_call(tokens, kv_gains, table, allowed, cotangent, w_query, w_out, ffn):
    z_size = lax.axis_size("z")
    own, width = tokens.shape
    seq = 2 * own
    rows, cols = w_query.shape
    head = table.shape[2] * 2
    units = ragged_split(ffn[0].shape[1], z_size)[1]
    low = lambda *dims: jax.ShapeDtypeStruct(dims, jnp.bfloat16)
    full = lambda *dims: jax.ShapeDtypeStruct(dims, jnp.float32)
    dma = lambda *lead: pltpu.SemaphoreType.DMA(lead)
    vmem = pl.BlockSpec(memory_space=pltpu.VMEM)
    hbm = pl.BlockSpec(memory_space=pl.ANY)
    wide = lambda *lead: pltpu.VMEM((*lead, width), jnp.bfloat16)
    return pl.pallas_call(
        functools.partial(pre_kernel, z_size),
        out_shape=(
            low(seq, width),
            low(seq, cols),
            low(seq, head),
            low(seq, head),
            low(seq, cols),
            full(own, width),
            low(seq, width),
            full(8, width),
            low(width, kv_gains.shape[1]),
            low(width, cols),
            low(width, cols),
            low(3, width, units),
            low(z_size, seq, width),
        ),
        in_specs=[vmem] * 4 + [hbm] * 6,
        out_specs=(vmem,) * 8 + (hbm,) * 5,
        scratch_shapes=[
            pltpu.VMEM((width, kv_gains.shape[1]), jnp.bfloat16),
            pltpu.VMEM((width, cols), jnp.bfloat16),
            pltpu.VMEM((width, cols), jnp.bfloat16),
            wide(seq),
            wide(seq),
            wide(own),
            pltpu.VMEM((seq, cols), jnp.float32),
            dma(4),
            dma(4),
            dma(3, z_size + 1),
            dma(3, z_size),
            dma(3, z_size),
            dma(3, z_size),
            dma(3, 2 * z_size),
            dma(3, 2 * z_size),
            dma(3, z_size, 2),
            dma(3, z_size, 2),
            dma(3, z_size),
            dma(3, z_size),
            dma(3, 2 * z_size),
            dma(3, 2 * z_size),
            dma(z_size),
            dma(z_size),
            dma(z_size),
            dma(z_size),
            dma(16),
        ],
        compiler_params=pltpu.CompilerParams(
            collective_id=1, has_side_effects=True, vmem_limit_bytes=VMEM_BYTES
        ),
        cost_estimate=pl.CostEstimate(
            flops=8 * seq * width * cols,
            bytes_accessed=8 * width * (cols + units),
            transcendentals=seq * seq * cols // head,
        ),
    )(tokens, kv_gains, table, allowed, cotangent, w_query, w_out, *ffn)


def norm_back(values, gain, upstream):
    scale = lax.rsqrt(jnp.mean(values * values, axis=-1, keepdims=True) + epsilon)
    normed = values * scale
    pulled = gain * upstream
    back = scale * (pulled - normed * jnp.mean(normed * pulled, axis=-1, keepdims=True))
    return back, jnp.sum(upstream * normed, axis=0, keepdims=True)


def post_kernel(
    z_size,
    mid_ref,
    tok_ref,
    cot_ref,
    gain_ref,
    n1_ref,
    rot_ref,
    key_ref,
    val_ref,
    att_ref,
    table_ref,
    allow_ref,
    kv_hbm,
    wq_hbm,
    wo_hbm,
    mix_hbm,
    gn_hbm,
    sums_hbm,
    mixed_ref,
    tgrad_ref,
    gsum_ref,
    kvg_ref,
    qg_ref,
    og_ref,
    ffn_out,
    kv_w,
    q_w,
    o_w,
    o_part,
    gm,
    gm_f,
    gq,
    gkv,
    kv_sum,
    back_y,
    mix_y,
    mix_z,
    mix_s,
    o_c,
    o_x,
    o_z,
    q_c,
    q_x,
    q_z,
    kv_y,
    kv_c,
    kv_x,
    kv_z,
    gain_own,
    gain_in,
    ffn_in,
    ffn_own,
    load_sem,
    own_sem,
    fx_send,
    fx_recv,
    fz_send,
    fz_recv,
    y_send,
    y_recv,
    my_send,
    my_recv,
    mz_send,
    mz_recv,
    wc_send,
    wc_recv,
    wx_send,
    wx_recv,
    wz_send,
    wz_recv,
    kc_send,
    kc_recv,
    kz_send,
    kz_recv,
    g_send,
    g_recv,
):
    me_z, me_x = lax.axis_index("z"), lax.axis_index("x")
    me_c, me_y = lax.axis_index("c"), lax.axis_index("mp")
    own, width = tok_ref.shape
    seq = 2 * own
    head = key_ref.shape[1]
    cols_here = att_ref.shape[1]
    heads = cols_here // head
    rows = qg_ref.shape[0]
    span = width // z_size
    mine = pl.ds(pl.multiple_of(me_y * own, own), own)
    theirs = pl.ds(pl.multiple_of((1 - me_y) * own, own), own)
    to_y, to_x, to_c = {"mp": 1 - me_y}, {"x": 1 - me_x}, {"c": 1 - me_c}
    head_scale = head ** (-0.5)

    def behind(step):
        return lax.rem(me_z - step + z_size, z_size)

    def to_z(step):
        return {"z": lax.rem(me_z + step, z_size)}

    def row_block(step, x_at, c_at):
        start = ((behind(step) * 2 + x_at) * 2 + c_at) * rows
        return pl.ds(pl.multiple_of(start, rows), rows)

    loads = [
        pltpu.make_async_copy(wo_hbm, o_w, load_sem.at[0]),
        pltpu.make_async_copy(wq_hbm, q_w, load_sem.at[1]),
        pltpu.make_async_copy(
            kv_hbm.at[:, :, :, :, :, pl.ds(0, 2 * head)], kv_w, load_sem.at[2]
        ),
    ]
    for step in range(z_size):
        loads.append(
            pltpu.make_async_copy(mix_hbm.at[step, mine], mix_s.at[step], load_sem.at[3 + step])
        )
    gn_load = pltpu.make_async_copy(gn_hbm, gm_f, load_sem.at[3 + z_size])
    gn_load.start()
    for load in loads:
        load.start()

    barrier = pltpu.get_barrier_semaphore()
    peers = [to_y, to_x, to_c] + [to_z(step) for step in range(1, z_size)]
    for where in peers:
        pl.semaphore_signal(barrier, inc=1, device_id=where, device_id_type=MESH_ID)
    pl.semaphore_wait(barrier, len(peers))

    tasks = [(step, kind) for step in (2, 3) for kind in range(3)]

    def f_x(index):
        step, kind = tasks[index]
        return remote(
            sums_hbm.at[kind, step, 1],
            ffn_in.at[index],
            fx_send.at[index],
            fx_recv.at[index],
            to_x,
        )

    def f_own(index):
        step, kind = tasks[index]
        return pltpu.make_async_copy(
            sums_hbm.at[kind, step, 0], ffn_own.at[index % 2], own_sem.at[index % 2]
        )

    def f_z(step, kind):
        if step == 1:
            src = sums_hbm.at[kind, 1, 0]
        else:
            src = ffn_in.at[tasks.index((step, kind))]
        return remote(
            src, ffn_out.at[kind, step], fz_send.at[kind, step], fz_recv.at[kind, step], to_z(step)
        )

    def tick(index):
        step, kind = tasks[index]
        f_x(index).wait_recv()
        f_own(index).wait()
        block = ffn_in.at[index]
        add_rows(block, [ffn_own.at[index % 2]], block, rows)
        if index + 2 < len(tasks):
            f_own(index + 2).start()
        f_z(step, kind).start()

    def f_x_own(kind):
        return remote(
            sums_hbm.at[kind, 0, 1],
            ffn_out.at[kind, 0],
            fx_send.at[len(tasks) + kind],
            fx_recv.at[len(tasks) + kind],
            to_x,
        )

    f_own(0).start()
    f_own(1).start()
    for index in range(len(tasks)):
        f_x(index).start()
    for kind in range(3):
        f_z(1, kind).start()
        f_x_own(kind).start()

    gn_load.wait()

    def mid_rows(index, total):
        at = pl.ds(pl.multiple_of(index * 32, 32), 32)
        grad, gain_part = norm_back(mid_ref[at, :], gain_ref[1:2, :], gm_f[at, :])
        grad = grad + cot_ref[at, :].astype(jnp.float32)
        gm_f[at, :] = grad
        gm[pl.ds(pl.multiple_of(me_y * own + index * 32, 32), 32), :] = grad.astype(jnp.bfloat16)
        return total + gain_part

    ffn_gain_part = lax.fori_loop(
        0, own // 32, mid_rows, jnp.zeros((1, width), jnp.float32)
    )
    gm_y = remote(gm.at[mine], gm.at[mine], y_send.at[0], y_recv.at[0], to_y)
    gm_y_in = remote(gm.at[theirs], gm.at[theirs], y_send.at[0], y_recv.at[0], to_y)
    gm_y.start()

    def mix_over_y(step):
        return remote(
            mix_hbm.at[step, theirs], mix_y.at[step], my_send.at[step], my_recv.at[step], to_y
        )

    def mix_over_z(step):
        return remote(
            mix_s.at[step], mix_z.at[step - 1], mz_send.at[step], mz_recv.at[step - 1], to_z(1)
        )

    def mix_step(step):
        mix_over_y(step).wait_recv()
        slot = (step - 2) % z_size
        others = [mix_y.at[step]]
        if step != 1:
            remote(
                mix_s.at[1], mix_z.at[slot], mz_send.at[1], mz_recv.at[slot], to_z(1)
            ).wait_recv()
            others.append(mix_z.at[slot])
        if step:
            add_rows(mix_s.at[step], others, mix_s.at[step], own)
            mix_over_z(step).start()
        else:
            add_rows(mid_ref, [mix_s.at[0], *others], mixed_ref, own)

    for step in (1, 2, 3, 0):
        mix_over_y(step).start()

    kinds = ((o_part, o_c, o_x, o_z, og_ref), (o_w, q_c, q_x, q_z, qg_ref))

    def w_c(kind, step, far):
        x_at = 1 - me_x if far else me_x
        return remote(
            kinds[kind][0].at[row_block(step, x_at, 1 - me_c)],
            kinds[kind][1].at[step, far],
            wc_send.at[kind, step, far],
            wc_recv.at[kind, step, far],
            to_c,
        )

    def w_x(kind, step):
        return remote(
            kinds[kind][0].at[row_block(step, 1 - me_x, me_c)],
            kinds[kind][2].at[step],
            wx_send.at[kind, step],
            wx_recv.at[kind, step],
            to_x,
        )

    first_z, last_z = (z_size - 1 - me_z) // (z_size - 1), me_z // (z_size - 1)
    inner = first_z + last_z == 0
    order = (
        0,
        1 + (me_z + 1) // 2,
        2 + (2 * me_z - 3) * (1 - first_z - last_z),
        3 - 2 * (me_z // 2),
    )
    right = (None, 1 - me_z // 2, (3 - me_z) * (2 - me_z) // 6 + me_z // 2 * (1 - last_z), 1 - me_z // 2)

    def w_z(kind, index):
        step, way = order[index], right[index]
        slot = way * lax.rem(step + 1, z_size) + (1 - way) * (step - 1 + 4 * ((3 - step) // 2))
        return remote(
            kinds[kind][0].at[row_block(step, me_x, me_c)],
            kinds[kind][3].at[slot],
            wz_send.at[kind, index],
            wz_recv.at[kind, slot],
            {"z": me_z + 2 * way - 1},
        )

    def w_z_in(kind, slot):
        block = kinds[kind][3].at[slot]
        return remote(block, block, wz_send.at[kind, 1], wz_recv.at[kind, slot], to_z(1))

    def w_x_stage(kind, index):
        step = order[index]
        w_c(kind, step, 1).wait_recv()
        block = kinds[kind][0].at[row_block(step, 1 - me_x, me_c)]
        add_rows(block, [kinds[kind][1].at[step, 1]], block, rows)
        w_x(kind, step).start()

    def w_z_stage(kind, index):
        part, from_c, from_x, from_z, result = kinds[kind]
        step = order[index]
        w_c(kind, step, 0).wait_recv()
        w_x(kind, step).wait_recv()
        block = part.at[row_block(step, me_x, me_c)]
        others = [from_c.at[step, 0], from_x.at[step]]
        if index:

            @pl.when(inner)
            def _():
                w_z_in(kind, step).wait_recv()
                add_rows(block, [*others, from_z.at[step]], block, rows)

            @pl.when(first_z + last_z > 0)
            def _():
                add_rows(block, others, block, rows)

            w_z(kind, index).start()
        else:

            @pl.when(first_z == 0)
            def _():
                w_z_in(kind, 0).wait_recv()

            @pl.when(last_z == 0)
            def _():
                w_z_in(kind, z_size).wait_recv()

            @pl.when(inner)
            def _():
                add_rows(block, [*others, from_z.at[0], from_z.at[z_size]], result, rows)

            @pl.when(first_z > 0)
            def _():
                add_rows(block, [*others, from_z.at[z_size]], result, rows)

            @pl.when(last_z > 0)
            def _():
                add_rows(block, [*others, from_z.at[0]], result, rows)

    def w_product(kind, index, left, values):
        step = order[index]
        at = pl.ds(pl.multiple_of(behind(step) * span, 128), span)
        turned = left[:, at].T

        def tile_body(tile, carry):
            cols = pl.ds(pl.multiple_of(tile * TILE, TILE), TILE)
            kinds[kind][0][at, cols] = dot_nn(turned, values[:, cols]).astype(jnp.bfloat16)
            return carry

        lax.fori_loop(0, cols_here // TILE, tile_body, 0)
        for far in (1, 0):
            w_c(kind, step, far).start()

    tick(0)
    tick(1)
    gm_y_in.wait_recv()
    w_product(0, 1, gm, att_ref)
    w_product(0, 2, gm, att_ref)
    w_x_stage(0, 1)
    w_product(0, 3, gm, att_ref)
    w_x_stage(0, 2)
    tick(2)
    w_product(0, 0, gm, att_ref)
    w_x_stage(0, 3)
    for load in loads:
        load.wait()

    kv_sum[...] = jnp.zeros(kv_sum.shape, jnp.float32)
    table = (table_ref[0], table_ref[1])

    for index in range(2):
        cols = pl.ds(index * (cols_here // 2), cols_here // 2)
        gq[:, cols] = dot_nn(gm[...], o_w[:, cols]).astype(jnp.bfloat16)

    def attend_back(index):
        cols = pl.ds(index * head, head)
        grad_vals = gq[:, cols]
        rotated = rot_ref[:, cols]
        probs = head_probs(rotated, key_ref[...], allow_ref[...])
        grad_probs = matmul_nt(grad_vals, val_ref[...])
        delta = jnp.sum(probs * grad_probs, axis=-1, keepdims=True)
        grad_scores = (probs * (grad_probs - delta)).astype(jnp.bfloat16)
        grad_rot = dot_nn(grad_scores, key_ref[...])
        gq[:, cols] = (spin_back(grad_rot, table) * head_scale).astype(jnp.bfloat16)
        kv_sum[0] += matmul_tn(grad_scores, rotated)
        kv_sum[1] += matmul_tn(probs.astype(jnp.bfloat16), grad_vals)

    for index in range(heads):
        attend_back(index)
        if index == 0:
            w_x_stage(0, 0)
        if 3 + index < len(tasks):
            tick(3 + index)
    gkv[:, :head] = spin_back(kv_sum[0], table).astype(jnp.bfloat16)
    gkv[:, head:] = kv_sum[1].astype(jnp.bfloat16)

    w_product(1, 1, n1_ref, gq)
    mix_step(1)
    w_product(1, 2, n1_ref, gq)
    w_x_stage(1, 1)
    w_z_stage(0, 1)
    w_product(1, 3, n1_ref, gq)
    w_x_stage(1, 2)
    w_product(1, 0, n1_ref, gq)
    w_x_stage(1, 3)
    w_x_stage(1, 0)
    mix_step(2)

    gm_y.wait_send()
    back = gm
    def input_tile(index, carry):
        at = pl.ds(pl.multiple_of(index * span, 128), span)
        back[:, at] = (
            matmul_nt(gq[...], q_w[at, :]) + matmul_nt(gkv[...], kv_w[index].reshape(span, 2 * head))
        ).astype(jnp.bfloat16)
        return carry

    lax.fori_loop(0, z_size, input_tile, 0)
    back_out = remote(back.at[theirs], back_y, y_send.at[1], y_recv.at[1], to_y)
    back_out.start()

    kv_part = kv_w

    def kv_tile(index, carry):
        at = pl.ds(pl.multiple_of(index * span, 128), span)
        product = dot_nn(n1_ref[:, at].T, gkv[...]).astype(jnp.bfloat16)
        kv_part[index] = product.reshape(kv_part.shape[1:])
        return carry

    lax.fori_loop(0, z_size, kv_tile, 0)
    kv_over_y = remote(kv_part.at[:, :, :, 1 - me_y], kv_y, y_send.at[2], y_recv.at[2], to_y)
    kv_over_y.start()
    w_z_stage(0, 2)
    mix_step(3)
    kv_over_y.wait_recv()

    def kv_add_y(index, carry):
        for x_at in range(2):
            for c_at in range(2):
                block = kv_part.at[index, x_at, c_at, me_y]
                block[...] = (
                    block[...].astype(jnp.float32) + kv_y[index, x_at, c_at].astype(jnp.float32)
                ).astype(jnp.bfloat16)
        return carry

    lax.fori_loop(0, z_size, kv_add_y, 0)
    kv_over_c = remote(
        kv_part.at[:, :, 1 - me_c, me_y], kv_c, kc_send.at[0], kc_recv.at[0], to_c
    )
    kv_over_c.start()
    w_z_stage(0, 3)
    w_z_stage(1, 1)
    kv_over_c.wait_recv()

    def kv_add_c(index, carry):
        for x_at in range(2):
            block = kv_part.at[index, x_at, me_c, me_y]
            block[...] = (
                block[...].astype(jnp.float32) + kv_c[index, x_at].astype(jnp.float32)
            ).astype(jnp.bfloat16)
        return carry

    lax.fori_loop(0, z_size, kv_add_c, 0)
    kv_over_x = remote(
        kv_part.at[:, 1 - me_x, me_c, me_y], kv_x, kc_send.at[1], kc_recv.at[1], to_x
    )
    kv_over_x.start()

    back_out.wait_recv()

    def input_rows(index, total):
        at = pl.ds(pl.multiple_of(index * 32, 32), 32)
        there = pl.ds(pl.multiple_of(me_y * own + index * 32, 32), 32)
        upstream = back[there, :].astype(jnp.float32) + back_y[at, :].astype(jnp.float32)
        grad, gain_part = norm_back(
            tok_ref[at, :].astype(jnp.float32), gain_ref[0:1, :], upstream
        )
        tgrad_ref[at, :] = (gm_f[at, :] + grad).astype(jnp.bfloat16)
        return total + gain_part

    attn_gain_part = lax.fori_loop(
        0, own // 32, input_rows, jnp.zeros((1, width), jnp.float32)
    )
    for index in range(4):
        at = slice(index * span, (index + 1) * span)
        gain_own[0, index : index + 1, :] = attn_gain_part[:, at]
        gain_own[0, 4 + index : 5 + index, :] = ffn_gain_part[:, at]

    def gain_send(stage, where):
        return remote(
            gain_own.at[stage], gain_in.at[stage], g_send.at[stage], g_recv.at[stage], where
        )

    gain_hops = [gain_send(0, to_y), gain_send(1, to_c), gain_send(2, to_x)]
    gain_last = [
        remote(
            gain_own.at[3], gain_in.at[2 + step], g_send.at[2 + step], g_recv.at[2 + step], to_z(step)
        )
        for step in range(1, z_size)
    ]

    def gain_fold(stage):
        gain_hops[stage].wait_recv()
        gain_own[stage + 1] = gain_own[stage] + gain_in[stage]

    gain_hops[0].start()
    mix_step(0)
    w_z_stage(0, 0)
    gain_fold(0)
    gain_hops[1].start()
    w_z_stage(1, 2)
    gain_fold(1)
    gain_hops[2].start()
    gain_fold(2)
    for copy in gain_last:
        copy.start()

    kv_over_x.wait_recv()

    def kv_add_x(index, carry):
        block = kv_part.at[index, me_x, me_c, me_y]
        block[...] = (
            block[...].astype(jnp.float32) + kv_x[index].astype(jnp.float32)
        ).astype(jnp.bfloat16)
        return carry

    lax.fori_loop(0, z_size, kv_add_x, 0)
    kv_over_z = [
        remote(
            kv_part.at[lax.rem(me_z + step, z_size), me_x, me_c, me_y],
            kv_z.at[step - 1],
            kz_send.at[step],
            kz_recv.at[step],
            to_z(step),
        )
        for step in range(1, z_size)
    ]
    for copy in kv_over_z:
        copy.start()
    w_z_stage(1, 3)
    for copy in gain_last:
        copy.wait_recv()
    gsum_ref[...] = gain_own[3] + gain_in[3] + gain_in[4] + gain_in[5]
    for copy in kv_over_z:
        copy.wait_recv()
    kvg_ref[...] = (
        kv_part[me_z, me_x, me_c, me_y].astype(jnp.float32)
        + kv_z[0].astype(jnp.float32)
        + kv_z[1].astype(jnp.float32)
        + kv_z[2].astype(jnp.float32)
    )
    w_z_stage(1, 0)

    back_out.wait_send()
    kv_over_y.wait_send()
    kv_over_c.wait_send()
    kv_over_x.wait_send()
    for kind in range(3):
        f_x_own(kind).wait()
    for index in range(len(tasks)):
        f_x(index).wait_send()
    for step in range(1, z_size):
        for kind in range(3):
            f_z(step, kind).wait()
    for copy in gain_hops + gain_last + kv_over_z:
        copy.wait_send()
    for step in range(z_size):
        mix_over_y(step).wait_send()
        if step:
            mix_over_z(step).wait_send()
        for kind in range(2):
            w_c(kind, step, 0).wait_send()
            w_c(kind, step, 1).wait_send()
            w_x(kind, step).wait_send()
            if step:
                w_z(kind, step).wait_send()


def post_call(
    grad_normed,
    mid,
    tokens,
    cotangent,
    gains,
    normed_one,
    rotated,
    keys,
    values,
    attn_vals,
    table,
    allowed,
    kv_weight,
    query_weight,
    out_weight,
    mix_parts,
    ffn_sums,
):
    z_size = lax.axis_size("z")
    own, width = tokens.shape
    seq = 2 * own
    head = keys.shape[1]
    cols = attn_vals.shape[1]
    rows = width // (4 * z_size)
    units = ffn_sums.shape[4]
    low = lambda *dims: pltpu.VMEM(dims, jnp.bfloat16)
    full = lambda *dims: pltpu.VMEM(dims, jnp.float32)
    out_full = lambda *dims: jax.ShapeDtypeStruct(dims, jnp.float32)
    out_low = lambda *dims: jax.ShapeDtypeStruct(dims, jnp.bfloat16)
    dma = lambda *lead: pltpu.SemaphoreType.DMA(lead)
    vmem = pl.BlockSpec(memory_space=pltpu.VMEM)
    hbm = pl.BlockSpec(memory_space=pl.ANY)
    z = z_size
    return pl.pallas_call(
        functools.partial(post_kernel, z_size),
        out_shape=(
            out_low(own, width),
            out_low(own, width),
            out_full(8, width // z),
            out_full(rows // 2, 2 * head),
            out_full(rows, cols),
            out_full(rows, cols),
            out_low(3, z, rows, units),
        ),
        in_specs=[vmem] * 11 + [hbm] * 6,
        out_specs=(vmem,) * 6 + (hbm,),
        scratch_shapes=[
            low(z, 2, 2, 2, rows // 2, 2 * head),
            low(width, cols),
            low(width, cols),
            low(width, cols),
            low(seq, width),
            full(own, width),
            low(seq, cols),
            low(seq, 2 * head),
            full(2, seq, head),
            low(own, width),
            low(z, own, width),
            low(z - 1, own, width),
            low(z, own, width),
            low(z, 2, rows, cols),
            low(z, rows, cols),
            low(z + 1, rows, cols),
            low(z, 2, rows, cols),
            low(z, rows, cols),
            low(z + 1, rows, cols),
            low(z, 2, 2, rows // 2, 2 * head),
            low(z, 2, rows // 2, 2 * head),
            low(z, rows // 2, 2 * head),
            low(z - 1, rows // 2, 2 * head),
            full(4, 8, width // z),
            full(6, 8, width // z),
            low(6, rows, units),
            low(2, rows, units),
            dma(4 + z),
            dma(2),
            dma(9),
            dma(9),
            dma(3, z),
            dma(3, z),
            dma(3),
            dma(3),
            dma(z),
            dma(z),
            dma(z),
            dma(z),
            dma(2, z, 2),
            dma(2, z, 2),
            dma(2, z),
            dma(2, z),
            dma(2, z),
            dma(2, z + 1),
            dma(2),
            dma(2),
            dma(z),
            dma(z),
            dma(6),
            dma(6),
        ],
        compiler_params=pltpu.CompilerParams(
            collective_id=2, has_side_effects=True, vmem_limit_bytes=VMEM_BYTES
        ),
        cost_estimate=pl.CostEstimate(
            flops=14 * seq * width * cols,
            bytes_accessed=10 * width * cols,
            transcendentals=seq * seq * cols // head,
        ),
    )(
        mid,
        tokens,
        cotangent,
        gains,
        normed_one,
        rotated,
        keys,
        values,
        attn_vals,
        table,
        allowed,
        kv_weight.reshape(z, 2, 2, 2, rows // 2, kv_weight.shape[1]),
        query_weight,
        out_weight,
        mix_parts,
        grad_normed,
        ffn_sums,
    )


def layout_kernel(
    z_size, main, sum_ref, ffn_ref, q_ref, o_ref, kv_ref, wg_ref, wu_ref, wd_ref, qg_ref, og_ref, kvg_ref
):
    me_z = lax.axis_index("z")
    for kind, out in enumerate((wg_ref, wu_ref, wd_ref)):
        out[:, z_size * main :] = jnp.zeros((out.shape[0], 64 * z_size), jnp.float32)
        for step in range(z_size):
            at = lax.rem(me_z - step + z_size, z_size)
            values = ffn_ref[kind, step].astype(jnp.float32)
            if step == 0:
                values = values + sum_ref[kind, 0, 0].astype(jnp.float32)
            body = pl.ds(pl.multiple_of(at * main, 128), main)
            out[:, body] = values[:, :main]
            tail = pl.ds(pl.multiple_of(z_size * main + at // 2 * 128, 128), 128)
            out[:, tail] += values[:, main:]
    qg_ref[...] = q_ref[...]
    og_ref[...] = o_ref[...]
    kvg_ref[...] = kv_ref[...]


def layout_call(ffn_sums, ffn_grads, query_grad, out_grad, kv_grad, ffn_cols):
    z_size = lax.axis_size("z")
    main, units = ragged_split(ffn_cols, z_size)
    rows, cols = query_grad.shape
    parts = rows // 32
    kv_rows = kv_grad.shape[0] // parts
    full = lambda *dims: jax.ShapeDtypeStruct(dims, jnp.float32)
    row = lambda height, width: pl.BlockSpec((height, width), lambda index: (index, 0))
    specs = [row(32, cols), row(32, cols), row(kv_rows, kv_grad.shape[1])]
    return pl.pallas_call(
        functools.partial(layout_kernel, z_size, main),
        grid=(parts,),
        out_shape=(
            *[full(rows, ffn_cols)] * 3,
            full(rows, cols),
            full(rows, cols),
            full(*kv_grad.shape),
        ),
        in_specs=[
            pl.BlockSpec((3, 1, 1, 32, units), lambda index: (0, 0, 0, index, 0)),
            pl.BlockSpec((3, z_size, 32, units), lambda index: (0, 0, index, 0)),
            *specs,
        ],
        out_specs=(*[row(32, ffn_cols)] * 3, *specs),
        compiler_params=pltpu.CompilerParams(vmem_limit_bytes=32 * 1024 * 1024),
    )(ffn_sums, ffn_grads, query_grad, out_grad, kv_grad)


FF_SPLIT = 4


def ffn_pass(normed, grad_out, gate_weight, up_weight, down_weight):
    gate = jnp.dot(normed, gate_weight, preferred_element_type=jnp.float32)
    up_proj = jnp.dot(normed, up_weight, preferred_element_type=jnp.float32)
    grad_hidden = jnp.dot(grad_out, down_weight, preferred_element_type=jnp.float32)
    product, pull = jax.vjp(gelu_product, gate, up_proj)
    hidden = product.astype(jnp.bfloat16)
    grad_gate_f, grad_up_f = pull(grad_hidden)
    grad_gate = grad_gate_f.astype(jnp.bfloat16)
    grad_up = grad_up_f.astype(jnp.bfloat16)
    mixed_part = matmul_nt(hidden, down_weight).astype(jnp.bfloat16)
    normed_part = (matmul_nt(grad_gate, gate_weight) + matmul_nt(grad_up, up_weight)).astype(
        jnp.bfloat16
    )
    weight_parts = [
        matmul_tn(normed, grad_gate).astype(jnp.bfloat16),
        matmul_tn(normed, grad_up).astype(jnp.bfloat16),
        matmul_tn(grad_out, hidden).astype(jnp.bfloat16),
    ]
    return mixed_part, normed_part, weight_parts


def shards_general(
    tokens,
    segments,
    positions,
    cotangent,
    attn_gain,
    ffn_gain,
    w_kv,
    w_query,
    w_out,
    w_gate,
    w_up,
    w_down,
):
    everywhere = ("z", "xc", "mp")
    dp = ("z", "xc")
    z_size = lax.axis_size("z")
    xc_size = lax.axis_size("xc")
    gains = lax.all_gather(
        jnp.stack([attn_gain, ffn_gain], axis=1), everywhere, axis=0, tiled=True
    ).astype(jnp.float32)
    gain_one, gain_two = gains[:, 0], gains[:, 1]
    kv_weight = lax.all_gather(w_kv, everywhere, axis=0, tiled=True)
    head_dim = kv_weight.shape[1] // 2
    width = tokens.shape[1]
    seq_len = segments.shape[0]
    heads_here = w_query.shape[1] // head_dim
    scale = head_dim ** (-0.5)
    cosine, sine = rotary_angles(positions, head_dim)
    inputs_f = tokens.astype(jnp.float32)
    tokens_all = lax.all_gather(tokens, "mp", axis=0, tiled=True)
    normed_one = norm_gain(tokens_all.astype(jnp.float32), gain_one).astype(jnp.bfloat16)
    query_weight = lax.all_gather(w_query, dp, axis=0, tiled=True)
    out_weight = lax.all_gather(w_out, dp, axis=0, tiled=True)

    rows = w_gate.shape[0]
    unit = w_gate.shape[1] // z_size

    def spread(weight):
        pieces = weight.reshape(rows, z_size, unit).transpose(1, 0, 2)
        pieces = lax.all_to_all(pieces, "z", split_axis=0, concat_axis=0, tiled=True)
        return lax.all_gather(pieces, "xc", axis=1, tiled=False).reshape(width, unit)

    gate_weight, up_weight, down_weight = spread(w_gate), spread(w_up), spread(w_down)
    grad_all = lax.all_gather(cotangent, ("z", "mp"), axis=0, tiled=True)

    query = jnp.dot(normed_one, query_weight, preferred_element_type=jnp.float32).reshape(
        seq_len, heads_here, head_dim
    )
    rotated = (rotate(query, cosine[:, None], sine[:, None]) * scale).astype(jnp.bfloat16)
    keyval = jnp.dot(normed_one, kv_weight, preferred_element_type=jnp.float32)
    keys = rotate(keyval[:, :head_dim], cosine, sine).astype(jnp.bfloat16)
    values = keyval[:, head_dim:].astype(jnp.bfloat16)
    allowed = block_allowed(segments, 0, seq_len)
    scores = jnp.einsum("thd,sd->hts", rotated, keys, preferred_element_type=jnp.float32)
    scores = jnp.where(allowed[None], scores, masked_score)
    row_max = jnp.max(scores, axis=-1, keepdims=True)
    weights = jnp.exp(scores - row_max)
    probs = weights / jnp.sum(weights, axis=-1, keepdims=True)
    probs_low = probs.astype(jnp.bfloat16)
    attn_vals = (
        jnp.einsum("hts,sd->thd", probs_low, values, preferred_element_type=jnp.float32)
        .reshape(seq_len, heads_here * head_dim)
        .astype(jnp.bfloat16)
    )
    mid = inputs_f + lax.psum_scatter(
        matmul_nt(attn_vals, out_weight).astype(jnp.bfloat16),
        "mp",
        scatter_dimension=0,
        tiled=True,
    ).astype(jnp.float32)
    normed_two = norm_gain(mid, gain_two).astype(jnp.bfloat16)
    normed_all = lax.all_gather(normed_two, ("z", "mp"), axis=0, tiled=True)

    mixed_part, normed_part, weight_parts = ffn_pass(
        normed_all, grad_all, gate_weight, up_weight, down_weight
    )
    grad_normed_two = lax.psum_scatter(
        normed_part, ("z", "mp"), scatter_dimension=0, tiled=True
    ).astype(jnp.float32)
    mixed = (
        mid
        + lax.psum_scatter(mixed_part, ("z", "mp"), scatter_dimension=0, tiled=True).astype(
            jnp.float32
        )
    ).astype(jnp.bfloat16)

    def collect(part):
        pieces = part.reshape(z_size, xc_size, rows, unit).transpose(1, 0, 2, 3)
        pieces = pieces.reshape(xc_size * z_size * rows, unit)
        pieces = lax.psum_scatter(pieces, "xc", scatter_dimension=0, tiled=True)
        pieces = pieces.reshape(z_size, rows, unit)
        pieces = lax.all_to_all(pieces, "z", split_axis=0, concat_axis=0, tiled=True)
        return pieces.transpose(1, 0, 2).reshape(rows, z_size * unit).astype(jnp.float32)

    w_gate_grad, w_up_grad, w_down_grad = [collect(part) for part in weight_parts]

    norm_pull_two = jax.vjp(norm_gain, mid, gain_two)[1]
    grad_mid_norm, grad_gain_two = norm_pull_two(grad_normed_two)
    grad_mid = cotangent.astype(jnp.float32) + grad_mid_norm
    grad_mid_all = lax.all_gather(grad_mid.astype(jnp.bfloat16), "mp", axis=0, tiled=True)
    grad_vals = (
        jnp.dot(grad_mid_all, out_weight, preferred_element_type=jnp.float32)
        .astype(jnp.bfloat16)
        .reshape(seq_len, heads_here, head_dim)
    )
    grad_probs = jnp.einsum("thd,sd->hts", grad_vals, values, preferred_element_type=jnp.float32)
    delta = jnp.sum(probs * grad_probs, axis=-1, keepdims=True)
    grad_scores = (probs * (grad_probs - delta)).astype(jnp.bfloat16)
    grad_rot = jnp.einsum("hts,sd->thd", grad_scores, keys, preferred_element_type=jnp.float32)
    key_sum = jnp.einsum("hts,thd->sd", grad_scores, rotated, preferred_element_type=jnp.float32)
    value_sum = jnp.einsum("hts,thd->sd", probs_low, grad_vals, preferred_element_type=jnp.float32)
    grad_query = (
        (unrotate(grad_rot, cosine[:, None], sine[:, None]) * scale)
        .reshape(seq_len, heads_here * head_dim)
        .astype(jnp.bfloat16)
    )
    grad_kv = jnp.concatenate([unrotate(key_sum, cosine, sine), value_sum], axis=1).astype(
        jnp.bfloat16
    )
    grad_normed_one = lax.psum_scatter(
        (matmul_nt(grad_query, query_weight) + matmul_nt(grad_kv, kv_weight)).astype(jnp.bfloat16),
        "mp",
        scatter_dimension=0,
        tiled=True,
    ).astype(jnp.float32)
    norm_pull_one = jax.vjp(norm_gain, inputs_f, gain_one)[1]
    grad_input_norm, grad_gain_one = norm_pull_one(grad_normed_one)
    tokens_grad = (grad_mid + grad_input_norm).astype(jnp.bfloat16)

    w_query_grad = lax.psum_scatter(
        matmul_tn(normed_one, grad_query).astype(jnp.bfloat16), dp, scatter_dimension=0, tiled=True
    ).astype(jnp.float32)
    w_out_grad = lax.psum_scatter(
        matmul_tn(grad_mid_all, attn_vals).astype(jnp.bfloat16), dp, scatter_dimension=0, tiled=True
    ).astype(jnp.float32)
    small = jnp.concatenate(
        [matmul_tn(normed_one, grad_kv), grad_gain_one[:, None], grad_gain_two[:, None]], axis=1
    )
    small = lax.psum_scatter(small, everywhere, scatter_dimension=0, tiled=True)
    kv_grad = small[:, : 2 * head_dim]
    return (
        mixed,
        tokens_grad,
        small[:, 2 * head_dim],
        small[:, 2 * head_dim + 1],
        kv_grad,
        w_query_grad,
        w_out_grad,
        w_gate_grad,
        w_up_grad,
        w_down_grad,
    )


def shards_fast(
    tokens,
    segments,
    positions,
    cotangent,
    attn_gain,
    ffn_gain,
    w_kv,
    w_query,
    w_out,
    w_gate,
    w_up,
    w_down,
):
    seq_len = segments.shape[0]
    cosine, sine = rotary_angles(positions, w_kv.shape[1] // 2)
    table = jnp.stack(
        [
            jnp.concatenate([cosine, cosine], axis=1),
            jnp.concatenate([-sine, sine], axis=1),
        ]
    )
    allowed = block_allowed(segments, 0, seq_len).astype(jnp.float32)
    kv_gains = jnp.concatenate(
        [w_kv, attn_gain[:, None], ffn_gain[:, None], jnp.zeros((w_kv.shape[0], 126), w_kv.dtype)],
        axis=1,
    )
    (
        normed_one,
        rotated,
        keys,
        values,
        attn_vals,
        mid,
        normed_two,
        gains,
        kv_weight,
        query_weight,
        out_weight,
        ffn_weights,
        grad_all,
    ) = pre_call(
        tokens, kv_gains, table, allowed, cotangent, w_query, w_out, (w_gate, w_up, w_down)
    )
    main = ragged_split(w_gate.shape[1], lax.axis_size("z"))[0]
    grad_normed_two, mix_parts, ffn_sums = ffn_call(
        normed_two, grad_all, ffn_weights, w_gate.shape[0], main
    )
    mixed, tokens_grad, gain_grads, kv_grad, query_grad, out_grad, ffn_grads = post_call(
        grad_normed_two,
        mid,
        tokens,
        cotangent,
        gains,
        normed_one,
        rotated,
        keys,
        values,
        attn_vals,
        table,
        allowed,
        kv_weight,
        query_weight,
        out_weight,
        mix_parts,
        ffn_sums,
    )
    *ffn_out, query_grad, out_grad, kv_grad = layout_call(
        ffn_sums, ffn_grads, query_grad, out_grad, kv_grad, w_gate.shape[1]
    )
    share = attn_gain.shape[0]
    place = lax.axis_index(("z", "x", "c", "mp")) * share
    gain_grads = gain_grads.reshape(2, gain_grads.size // 2)
    gain_grads = lax.dynamic_slice(gain_grads, (0, place), (2, share))
    return (
        mixed,
        tokens_grad,
        gain_grads[0],
        gain_grads[1],
        kv_grad,
        query_grad,
        out_grad,
        *ffn_out,
    )


def solution(mesh):
    dp_size, mp_size = mesh.shape["dp"], mesh.shape["mp"]
    if dp_size == 4 * FF_SPLIT and mp_size == 2:
        body, dp = shards_fast, ("z", "x", "c")
        sizes = (FF_SPLIT, 2, 2, mp_size)
    else:
        body, dp = shards_general, ("z", "xc")
        sizes = (FF_SPLIT, dp_size // FF_SPLIT, mp_size)
    all_axes = (*dp, "mp")
    fine = jax.sharding.Mesh(mesh.devices.reshape(sizes), all_axes)
    in_specs = (
        P(all_axes, None),
        P(dp),
        P(dp),
        P(all_axes, None),
        P(all_axes),
        P(all_axes),
        P(all_axes, None),
        P(dp, "mp"),
        P(dp, "mp"),
        P(dp, "mp"),
        P(dp, "mp"),
        P(dp, "mp"),
    )
    out_specs = (
        P(all_axes, None),
        P(all_axes, None),
        P(all_axes),
        P(all_axes),
        P(all_axes, None),
        P(dp, "mp"),
        P(dp, "mp"),
        P(dp, "mp"),
        P(dp, "mp"),
        P(dp, "mp"),
    )
    return jax.shard_map(body, mesh=fine, in_specs=in_specs, out_specs=out_specs, check_vma=False)
```

```python
import functools

import jax
import jax.numpy as jnp
from jax import lax
from jax.experimental import pallas as pl
from jax.experimental.pallas import tpu as pltpu
from jax.sharding import PartitionSpec as P

WINDOW = 2048


epsilon = 1e-06
rope_base = 10000.0
masked_score = -1e30
VMEM_BYTES = 66_000_000


def norm_gain(values, gain):
    return values * lax.rsqrt(jnp.mean(values * values, axis=-1, keepdims=True) + epsilon) * gain


def rotary_angles(positions, head_width):
    quarter = head_width // 4
    freqs = rope_base ** (-jnp.arange(quarter).astype(jnp.float32) / quarter)
    phase = positions.astype(jnp.float32)[:, None] * freqs[None, :]
    return (jnp.cos(phase), jnp.sin(phase))


def rotate(values, cosine, sine):
    quarter = cosine.shape[-1]
    first_half = values[..., :quarter]
    second_half = values[..., quarter : 2 * quarter]
    return jnp.concatenate(
        [
            first_half * cosine - second_half * sine,
            second_half * cosine + first_half * sine,
            values[..., 2 * quarter :],
        ],
        axis=-1,
    )


def unrotate(values, cosine, sine):
    quarter = cosine.shape[-1]
    first_half = values[..., :quarter]
    second_half = values[..., quarter : 2 * quarter]
    return jnp.concatenate(
        [
            first_half * cosine + second_half * sine,
            second_half * cosine - first_half * sine,
            values[..., 2 * quarter :],
        ],
        axis=-1,
    )


def gelu_product(gate, up_proj):
    return jax.nn.gelu(gate, approximate=True) * up_proj


def matmul_nt(left, right):
    return lax.dot_general(
        left, right, (((1,), (1,)), ((), ())), preferred_element_type=jnp.float32
    )


def matmul_tn(left, right):
    return lax.dot_general(
        left, right, (((0,), (0,)), ((), ())), preferred_element_type=jnp.float32
    )


def block_allowed(segments, first_row, rows):
    seq_len = segments.shape[0]
    query_rows = first_row + jnp.arange(rows)
    key_rows = jnp.arange(seq_len)
    return (
        (segments[:, None] == segments[None, :])
        & (key_rows[None, :] <= query_rows[:, None])
        & (query_rows[:, None] - key_rows[None, :] < WINDOW)
    )


MESH_ID = pl.DeviceIdType.MESH
GELU_A = 0.7978845608028654
GELU_B = 0.044715
TILE = 256
WIDE = 512


def remote(src, dst, send_sem, recv_sem, where):
    return pltpu.make_async_remote_copy(
        src_ref=src,
        dst_ref=dst,
        send_sem=send_sem,
        recv_sem=recv_sem,
        device_id=where,
        device_id_type=MESH_ID,
    )


def dot_nn(left, right):
    return lax.dot_general(
        left, right, (((1,), (0,)), ((), ())), preferred_element_type=jnp.float32
    )


def gelu_parts(gate):
    square = gate * gate
    bend = jnp.tanh(GELU_A * gate * (1.0 + GELU_B * square))
    half = 0.5 * (1.0 + bend)
    slope = half + 0.5 * gate * (1.0 - bend * bend) * GELU_A * (1.0 + 3.0 * GELU_B * square)
    return gate * half, slope


def add_rows(first, rest, out, count):
    def body(index, carry):
        step = pl.ds(pl.multiple_of(index * 32, 32), 32)
        total = first[step, :].astype(jnp.float32)
        for other in rest:
            total = total + other[step, :].astype(jnp.float32)
        out[step, :] = total.astype(out.dtype)
        return carry

    lax.fori_loop(0, count // 32, body, 0)


def ffn_kernel(
    z_size,
    main,
    own_ref,
    dy_hbm,
    w_hbm,
    gn_ref,
    mix_hbm,
    sums_hbm,
    n2,
    dy,
    w3,
    h3,
    left_t,
    gn_part,
    mix_buf,
    gn_y,
    gn_z,
    gn_s,
    c_in,
    x_in,
    load_sem,
    mix_sem,
    ag_y_send,
    ag_y_recv,
    ag_z_send,
    ag_z_recv,
    rs_y_send,
    rs_y_recv,
    rs_z_send,
    rs_z_recv,
    c_send,
    c_recv,
    x_send,
    x_recv,
    out_sem,
):
    own = own_ref.shape[0] // 2
    width = own_ref.shape[1]
    units = w3.shape[2]
    rows = c_in.shape[3]
    span = width // z_size
    me_y, me_z = lax.axis_index("mp"), lax.axis_index("z")
    me_x, me_c = lax.axis_index("x"), lax.axis_index("c")
    mine = pl.ds(pl.multiple_of(me_y * own, own), own)
    theirs = pl.ds(pl.multiple_of((1 - me_y) * own, own), own)
    to_y, to_x, to_c = {"mp": 1 - me_y}, {"x": 1 - me_x}, {"c": 1 - me_c}

    def ahead(step):
        return lax.rem(me_z + step, z_size)

    def to_z(step):
        return {"z": ahead(step)}

    def row_block(z_at, x_at, c_at):
        return pl.ds(pl.multiple_of(((z_at * 2 + x_at) * 2 + c_at) * rows, rows), rows)

    loads = []
    for index in range(z_size):
        loads.append(pltpu.make_async_copy(dy_hbm.at[index], dy.at[index], load_sem.at[index]))
    for index in range(3):
        loads.append(
            pltpu.make_async_copy(w_hbm.at[index], w3.at[index], load_sem.at[z_size + index])
        )
    for load in loads:
        load.start()

    barrier = pltpu.get_barrier_semaphore()
    peers = [to_y, to_x, to_c] + [to_z(step) for step in range(1, z_size)]
    for where in peers:
        pl.semaphore_signal(barrier, inc=1, device_id=where, device_id_type=MESH_ID)
    pl.semaphore_wait(barrier, len(peers))

    def ag_y(index):
        block = n2.at[index, mine]
        return remote(block, block, ag_y_send.at[index], ag_y_recv.at[index], to_y)

    def ag_y_in(index):
        block = n2.at[index, theirs]
        return remote(block, block, ag_y_send.at[index], ag_y_recv.at[index], to_y)

    def ag_z(index):
        src = own_ref.at[mine] if index == 0 else n2.at[index, mine]
        return remote(
            src, n2.at[index + 1, mine], ag_z_send.at[index], ag_z_recv.at[index + 1], to_z(1)
        )

    def ag_z_in(index):
        block = n2.at[index, mine]
        return remote(block, block, ag_z_send.at[0], ag_z_recv.at[index], to_z(1))

    def forward(index):
        ag_z_in(index).wait_recv()
        if index < z_size - 1:
            ag_z(index).start()
        ag_y(index).start()

    ag_z(0).start()
    n2[0] = own_ref[...]

    mix_copies = []

    def chunk(first, count, between=None):
        for index in range(first, first + count):
            if index:
                ag_y_in(index).wait_recv()
            if index >= 2:
                mix_copies[index - 2].wait()
        rows_at = pl.ds(first * 2 * own, count * 2 * own)

        def up_tile(tile, carry):
            cols = pl.ds(pl.multiple_of(tile * TILE, TILE), TILE)

            def product(left, kind):
                values = left[first : first + count].reshape(count * 2 * own, width)
                return dot_nn(values, w3[kind, :, cols])

            gate = product(n2, 0)
            up_proj = product(n2, 1)
            grad_hidden = product(dy, 2)
            act, slope = gelu_parts(gate)
            at = lax.broadcasted_iota(jnp.int32, (1, TILE), 1) + tile * TILE
            low_at = main + 64 * lax.rem(me_z, 2)
            keep = (at < main) | ((at >= low_at) & (at < low_at + 64))
            act = jnp.where(keep, act, 0.0)
            slope = jnp.where(keep, slope, 0.0)
            h3[0, rows_at, cols] = (grad_hidden * up_proj * slope).astype(jnp.bfloat16)
            h3[1, rows_at, cols] = (grad_hidden * act).astype(jnp.bfloat16)
            h3[2, rows_at, cols] = (act * up_proj).astype(jnp.bfloat16)
            return carry

        lax.fori_loop(0, units // TILE, up_tile, 0)
        if between:
            between()

        for index in range(first, first + count):
            here = pl.ds(index * 2 * own, 2 * own)

            def down_tile(tile, carry, index=index, here=here):
                at = pl.ds(pl.multiple_of(tile * 2 * span, 128), 2 * span)
                normed = matmul_nt(w3[0, at, :], h3[0, here, :]) + matmul_nt(
                    w3[1, at, :], h3[1, here, :]
                )
                mixed = matmul_nt(w3[2, at, :], h3[2, here, :])
                for half in range(2):
                    cols = slice(half * own, (half + 1) * own)
                    gn_part[index, half, at, :] = normed[:, cols].astype(jnp.bfloat16)
                    mix_buf[index % 2, half, at, :] = mixed[:, cols].astype(jnp.bfloat16)
                return carry

            lax.fori_loop(0, z_size // 2, down_tile, 0)
            copy = pltpu.make_async_copy(
                mix_buf.at[index % 2], mix_hbm.at[index], mix_sem.at[index]
            )
            copy.start()
            mix_copies.append(copy)

    def rs_y(index):
        return remote(
            gn_part.at[index, 1 - me_y], gn_y.at[index], rs_y_send.at[index], rs_y_recv.at[index], to_y
        )

    def rs_z(index):
        return remote(
            gn_s.at[index - 1],
            gn_z.at[index - 1],
            rs_z_send.at[index],
            rs_z_recv.at[index - 1],
            to_z(1),
        )

    def rs_step(index):
        rs_y(index).wait_recv()
        slot = (index - 2) % z_size
        if index != 1:
            remote(
                gn_s.at[slot], gn_z.at[slot], rs_z_send.at[1], rs_z_recv.at[slot], to_z(1)
            ).wait_recv()

        def add_tile(tile, carry):
            at = pl.ds(pl.multiple_of(tile * TILE, TILE), TILE)
            total = gn_part[index, me_y, at, :].astype(jnp.float32) + gn_y[index, at, :].astype(
                jnp.float32
            )
            if index != 1:
                total = total + gn_z[slot, at, :].astype(jnp.float32)
            if index == 0:
                gn_ref[:, at] = total.T
            else:
                gn_s[index - 1, at, :] = total.astype(jnp.bfloat16)
            return carry

        lax.fori_loop(0, width // TILE, add_tile, 0)
        if index != 0:
            rs_z(index).start()


    def grads(step):
        at = pl.ds(pl.multiple_of(ahead(step) * span, 128), span)
        for kinds, source in (((0, 1), n2), ((2,), dy)):
            left_t[...] = source[:, :, at].reshape(z_size * 2 * own, span).T
            for kind in kinds:

                def tile_body(tile, carry, kind=kind):
                    cols = pl.ds(pl.multiple_of(tile * WIDE, WIDE), WIDE)
                    w3[kind, at, cols] = dot_nn(left_t[...], h3[kind, :, cols]).astype(jnp.bfloat16)
                    return carry

                lax.fori_loop(0, units // WIDE, tile_body, 0)
        for far in (1, 0):
            for kind in range(3):
                over_c(kind, step, far).start()

    def over_c(kind, step, far):
        x_at = 1 - me_x if far else me_x
        return remote(
            w3.at[kind, row_block(ahead(step), x_at, 1 - me_c)],
            c_in.at[kind, step, far],
            c_send.at[kind, step, far],
            c_recv.at[kind, step, far],
            to_c,
        )

    def over_x(kind):
        return remote(
            w3.at[kind, row_block(ahead(1), 1 - me_x, me_c)],
            x_in.at[kind],
            x_send.at[kind],
            x_recv.at[kind],
            to_x,
        )

    out_copies = []

    def keep(kind, step, far, block):
        copy = pltpu.make_async_copy(
            block, sums_hbm.at[kind, step, far], out_sem.at[kind, step, far]
        )
        copy.start()
        out_copies.append(copy)

    def core_sums(step):
        for far in (1, 0):
            for kind in range(3):
                over_c(kind, step, far).wait_recv()
                x_at = 1 - me_x if far else me_x
                block = w3.at[kind, row_block(ahead(step), x_at, me_c)]
                add_rows(block, [c_in.at[kind, step, far]], block, rows)
                if step != 1:
                    keep(kind, step, far, block)
                elif far:
                    over_x(kind).start()

    def first_sums():
        for kind in range(3):
            over_x(kind).wait_recv()
            block = w3.at[kind, row_block(ahead(1), me_x, me_c)]
            add_rows(block, [x_in.at[kind]], block, rows)
            keep(kind, 1, 0, block)

    forward(1)
    for load in loads:
        load.wait()
    chunk(0, 1)
    rs_y(0).start()
    forward(2)
    chunk(1, 1)
    rs_y(1).start()
    forward(3)
    chunk(2, 2, lambda: rs_step(1))
    rs_y(2).start()
    rs_y(3).start()
    grads(1)
    rs_step(2)
    grads(2)
    core_sums(1)
    rs_step(3)
    grads(3)
    core_sums(2)
    grads(0)
    core_sums(3)
    rs_step(0)
    core_sums(0)
    first_sums()

    for copy in mix_copies[2:] + out_copies:
        copy.wait()
    for index in range(z_size):
        if index:
            ag_y(index).wait_send()
        rs_y(index).wait_send()
        if index < z_size - 1:
            ag_z(index).wait_send()
        if index:
            rs_z(index).wait_send()
        for kind in range(3):
            over_c(kind, index, 0).wait_send()
            over_c(kind, index, 1).wait_send()
            if index == 1:
                over_x(kind).wait_send()


def ffn_call(normed, grad_all, weights, rows, main):
    z_size = lax.axis_size("z")
    pair, width = normed.shape
    units = weights.shape[2]
    own = pair // 2
    wide = lambda *lead: pltpu.VMEM((*lead, width), jnp.bfloat16)
    tall = lambda *lead: pltpu.VMEM((*lead, width, own), jnp.bfloat16)
    dma = lambda *lead: pltpu.SemaphoreType.DMA(lead)
    vmem = pl.BlockSpec(memory_space=pltpu.VMEM)
    hbm = pl.BlockSpec(memory_space=pl.ANY)
    return pl.pallas_call(
        functools.partial(ffn_kernel, z_size, main),
        out_shape=(
            jax.ShapeDtypeStruct((own, width), jnp.float32),
            jax.ShapeDtypeStruct((z_size, 2, width, own), jnp.bfloat16),
            jax.ShapeDtypeStruct((3, z_size, 2, rows, units), jnp.bfloat16),
        ),
        in_specs=[vmem, hbm, hbm],
        out_specs=(vmem, hbm, hbm),
        scratch_shapes=[
            wide(z_size, pair),
            wide(z_size, pair),
            pltpu.VMEM(weights.shape, jnp.bfloat16),
            pltpu.VMEM((3, z_size * pair, units), jnp.bfloat16),
            pltpu.VMEM((width // z_size, z_size * pair), jnp.bfloat16),
            tall(z_size, 2),
            tall(2, 2),
            tall(z_size),
            tall(z_size - 1),
            tall(z_size - 1),
            pltpu.VMEM((3, z_size, 2, rows, units), jnp.bfloat16),
            pltpu.VMEM((3, rows, units), jnp.bfloat16),
            dma(z_size + 3),
            dma(z_size),
            dma(z_size),
            dma(z_size),
            dma(z_size),
            dma(z_size),
            dma(z_size),
            dma(z_size),
            dma(z_size),
            dma(z_size),
            dma(3, z_size, 2),
            dma(3, z_size, 2),
            dma(3),
            dma(3),
            dma(3, z_size, 2),
        ],
        compiler_params=pltpu.CompilerParams(
            collective_id=0, has_side_effects=True, vmem_limit_bytes=VMEM_BYTES
        ),
        cost_estimate=pl.CostEstimate(
            flops=18 * z_size * pair * width * units,
            bytes_accessed=4 * weights.size + 12 * z_size * pair * width,
            transcendentals=z_size * pair * units,
        ),
    )(normed, grad_all, weights)


def spin(values, table):
    first = values[:, : values.shape[1] // 2]
    turned = first * table[0] + pltpu.roll(first, first.shape[1] // 2, 1) * table[1]
    return jnp.concatenate([turned, values[:, values.shape[1] // 2 :]], axis=1)


def spin_back(values, table):
    first = values[:, : values.shape[1] // 2]
    turned = first * table[0] - pltpu.roll(first, first.shape[1] // 2, 1) * table[1]
    return jnp.concatenate([turned, values[:, values.shape[1] // 2 :]], axis=1)


def head_probs(rotated, keys, allowed):
    scores = jnp.where(allowed > 0.5, matmul_nt(rotated, keys), masked_score)
    weights = jnp.exp(scores - jnp.max(scores, axis=-1, keepdims=True))
    return weights / jnp.sum(weights, axis=-1, keepdims=True)


def ragged_split(columns, parts):
    main = columns // parts // 128 * 128
    return main, main + 128


def pre_kernel(
    z_size,
    tok_ref,
    kvg_ref,
    table_ref,
    allow_ref,
    cot_hbm,
    wq_hbm,
    wo_hbm,
    wg_hbm,
    wu_hbm,
    wd_hbm,
    n1_ref,
    rot_ref,
    key_ref,
    val_ref,
    att_ref,
    mid_ref,
    n2_ref,
    gain_ref,
    kv_out,
    wq_out,
    wo_out,
    w3_out,
    dy_out,
    kv_w,
    q_w,
    o_w,
    tok,
    part,
    part_y,
    query,
    y_send,
    y_recv,
    az_send,
    az_recv,
    ax_send,
    ax_recv,
    ac_send,
    ac_recv,
    fz_send,
    fz_recv,
    fx_send,
    fx_recv,
    fc_send,
    fc_recv,
    dz_send,
    dz_recv,
    dy_send,
    dy_recv,
    local_sem,
):
    me_z, me_x = lax.axis_index("z"), lax.axis_index("x")
    me_c, me_y = lax.axis_index("c"), lax.axis_index("mp")
    own, width = tok_ref.shape
    rows = wq_hbm.shape[0]
    half_rows = kvg_ref.shape[0]
    head = key_ref.shape[1]
    main, units = ragged_split(wg_hbm.shape[1], z_size)
    to_y, to_x, to_c = {"mp": 1 - me_y}, {"x": 1 - me_x}, {"c": 1 - me_c}

    def to_z(step):
        return {"z": lax.rem(me_z + step, z_size)}

    def from_z(step):
        return lax.rem(me_z - step + z_size, z_size)

    def row_block(step, x_at, c_at):
        start = ((from_z(step) * 2 + x_at) * 2 + c_at) * rows
        return pl.ds(pl.multiple_of(start, rows), rows)

    mine = pl.ds(pl.multiple_of(me_y * own, own), own)
    theirs = pl.ds(pl.multiple_of((1 - me_y) * own, own), own)
    bufs = (kv_w, q_w, o_w)
    inputs = (None, wq_hbm, wo_hbm)

    locals_ = []

    def local(src, dst):
        copy = pltpu.make_async_copy(src, dst, local_sem.at[len(locals_)])
        copy.start()
        locals_.append(copy)
        return copy

    here = row_block(0, me_x, me_c)
    own_q = local(wq_hbm, q_w.at[here])
    own_o = local(wo_hbm, o_w.at[here])
    ffn_in = (wg_hbm, wu_hbm, wd_hbm)

    def pieces(target):
        yield pl.ds(pl.multiple_of(target * main, 128), main), pl.ds(0, main)
        tail = (z_size * main) + (target // 2) * 128
        yield pl.ds(pl.multiple_of(tail, 128), 128), pl.ds(main, 128)

    own_f = []
    for kind in range(3):
        for src, dst in pieces(me_z):
            own_f.append(local(ffn_in[kind].at[:, src], w3_out.at[kind, here, dst]))
    own_d = local(cot_hbm, dy_out.at[0, mine])

    barrier = pltpu.get_barrier_semaphore()
    peers = [to_y, to_x, to_c] + [to_z(step) for step in range(1, z_size)]
    for where in peers:
        pl.semaphore_signal(barrier, inc=1, device_id=where, device_id_type=MESH_ID)
    pl.semaphore_wait(barrier, len(peers))

    kv_mine = pl.ds(pl.multiple_of(here.start + me_y * half_rows, half_rows), half_rows)
    kv_theirs = pl.ds(pl.multiple_of(here.start + (1 - me_y) * half_rows, half_rows), half_rows)
    kv_y = remote(kvg_ref, kv_w.at[kv_mine], y_send.at[0], y_recv.at[0], to_y)
    kv_y_in = remote(kvg_ref, kv_w.at[kv_theirs], y_send.at[0], y_recv.at[0], to_y)
    tok_y = remote(tok_ref, tok.at[mine], y_send.at[1], y_recv.at[1], to_y)
    tok_y_in = remote(tok_ref, tok.at[theirs], y_send.at[1], y_recv.at[1], to_y)
    part_out = remote(part.at[theirs], part_y, y_send.at[2], y_recv.at[2], to_y)
    n2_y = remote(n2_ref.at[mine], n2_ref.at[mine], y_send.at[3], y_recv.at[3], to_y)
    n2_y_in = remote(n2_ref.at[theirs], n2_ref.at[theirs], y_send.at[3], y_recv.at[3], to_y)

    def source(kind, step):
        if isinstance(step, int) and step == 0 and kind:
            return inputs[kind]
        return bufs[kind].at[row_block(step, me_x, me_c)]

    first_z, last_z = (z_size - 1 - me_z) // (z_size - 1), me_z // (z_size - 1)
    inner = first_z + last_z == 0
    order = (0, 1 + 2 * first_z, 3 - first_z - last_z, 2 - first_z + last_z)
    hops = (
        None,
        (lax.rem(me_z + 1, z_size), 2),
        (lax.rem(me_z + z_size - 1, z_size), 2),
        (lax.rem(3 * (me_z + 3), z_size), lax.rem(2 * me_z + 3, z_size)),
    )

    def a_z_own(kind, right):
        return remote(
            source(kind, 0),
            bufs[kind].at[here],
            az_send.at[kind, right],
            az_recv.at[kind, 1 if right else z_size - 1],
            to_z(1 if right else z_size - 1),
        )

    def a_z_start(kind):
        @pl.when(last_z == 0)
        def _():
            a_z_own(kind, 1).start()

        @pl.when(first_z == 0)
        def _():
            a_z_own(kind, 0).start()

    def a_z(kind, index):
        target, slot = hops[index]
        block = bufs[kind].at[row_block(order[index], me_x, me_c)]
        return remote(
            block, block, az_send.at[kind, 1 + index], az_recv.at[kind, slot], {"z": target}
        )

    def a_z_next(kind, index):
        @pl.when(inner)
        def _():
            a_z(kind, index).start()

    def a_z_done(kind):
        @pl.when(last_z == 0)
        def _():
            a_z_own(kind, 1).wait_send()

        @pl.when(first_z == 0)
        def _():
            a_z_own(kind, 0).wait_send()

        @pl.when(inner)
        def _():
            for index in range(1, z_size):
                a_z(kind, index).wait_send()

    def a_z_in(kind, step):
        block = bufs[kind].at[row_block(step, me_x, me_c)]
        return remote(block, block, az_send.at[kind, 0], az_recv.at[kind, step], to_z(1))

    def a_x(kind, step):
        return remote(
            source(kind, step),
            bufs[kind].at[row_block(step, me_x, me_c)],
            ax_send.at[kind, step],
            ax_recv.at[kind, step],
            to_x,
        )

    def a_x_in(kind, step):
        block = bufs[kind].at[row_block(step, 1 - me_x, me_c)]
        return remote(block, block, ax_send.at[kind, step], ax_recv.at[kind, step], to_x)

    def a_c(kind, step, far):
        x_at = 1 - me_x if far else me_x
        block = bufs[kind].at[row_block(step, x_at, me_c)]
        src = block if far else source(kind, step)
        slot = step + z_size * far
        return remote(src, block, ac_send.at[kind, slot], ac_recv.at[kind, slot], to_c)

    def a_c_in(kind, step, far):
        x_at = 1 - me_x if far else me_x
        block = bufs[kind].at[row_block(step, x_at, 1 - me_c)]
        slot = step + z_size * far
        return remote(block, block, ac_send.at[kind, slot], ac_recv.at[kind, slot], to_c)

    def f_z(kind, step):
        target = lax.rem(me_z + step, z_size)
        return [
            remote(
                ffn_in[kind].at[:, src],
                w3_out.at[kind, here, dst],
                fz_send.at[kind, step, index],
                fz_recv.at[kind, step, index],
                to_z(step),
            )
            for index, (src, dst) in enumerate(pieces(target))
        ]

    def f_z_in(kind, step):
        block = row_block(step, me_x, me_c)
        return [
            remote(
                w3_out.at[kind, block, dst],
                w3_out.at[kind, block, dst],
                fz_send.at[kind, step, index],
                fz_recv.at[kind, step, index],
                to_z(step),
            )
            for index, (_, dst) in enumerate(pieces(me_z))
        ]

    def f_x(kind, step):
        block = w3_out.at[kind, row_block(step, me_x, me_c)]
        return remote(block, block, fx_send.at[kind, step], fx_recv.at[kind, step], to_x)

    def f_x_in(kind, step):
        block = w3_out.at[kind, row_block(step, 1 - me_x, me_c)]
        return remote(block, block, fx_send.at[kind, step], fx_recv.at[kind, step], to_x)

    def f_c(kind, step, far):
        block = w3_out.at[kind, row_block(step, 1 - me_x if far else me_x, me_c)]
        slot = step + z_size * far
        return remote(block, block, fc_send.at[kind, slot], fc_recv.at[kind, slot], to_c)

    def f_c_in(kind, step, far):
        block = w3_out.at[kind, row_block(step, 1 - me_x if far else me_x, 1 - me_c)]
        slot = step + z_size * far
        return remote(block, block, fc_send.at[kind, slot], fc_recv.at[kind, slot], to_c)

    def d_source(step):
        return cot_hbm if isinstance(step, int) else dy_out.at[step, mine]

    def d_z_own(right):
        slot = 1 if right else z_size - 1
        return remote(
            cot_hbm, dy_out.at[slot, mine], dz_send.at[right], dz_recv.at[slot], to_z(slot)
        )

    def d_z_start():
        @pl.when(last_z == 0)
        def _():
            d_z_own(1).start()

        @pl.when(first_z == 0)
        def _():
            d_z_own(0).start()

    def d_z(index):
        target, slot = hops[index]
        return remote(
            dy_out.at[order[index], mine],
            dy_out.at[slot, mine],
            dz_send.at[1 + index],
            dz_recv.at[slot],
            {"z": target},
        )

    def d_z_done():
        @pl.when(last_z == 0)
        def _():
            d_z_own(1).wait_send()

        @pl.when(first_z == 0)
        def _():
            d_z_own(0).wait_send()

        @pl.when(inner)
        def _():
            for index in range(1, z_size):
                d_z(index).wait_send()

    def d_z_in(step):
        block = dy_out.at[step, mine]
        return remote(block, block, dz_send.at[0], dz_recv.at[step], to_z(1))

    def d_y(step):
        return remote(
            d_source(step), dy_out.at[step, mine], dy_send.at[step], dy_recv.at[step], to_y
        )

    def d_y_in(step):
        block = dy_out.at[step, theirs]
        return remote(block, block, dy_send.at[step], dy_recv.at[step], to_y)

    kv_y.start()
    tok_y.start()
    for kind in (1, 2):
        a_z_start(kind)
        a_x(kind, 0).start()
        a_c(kind, 0, 0).start()
    kv_w[kv_mine, :] = kvg_ref[...]
    tok[mine, :] = tok_ref[...]
    kv_y_in.wait_recv()
    a_z_start(0)
    a_x(0, 0).start()
    a_c(0, 0, 0).start()
    d_y(0).start()
    for step in range(1, z_size):
        for kind in (1, 0, 2):
            a_z_in(kind, order[step]).wait_recv()
            a_z_next(kind, step)
            a_x(kind, order[step]).start()
            a_c(kind, order[step], 0).start()
        if step == z_size - 2:
            d_z_start()
        if step == z_size - 1:
            for copy in own_f:
                copy.wait()
            for kind in range(3):
                for away in (1, 3, 2):
                    for copy in f_z(kind, away):
                        copy.start()
            for kind in range(3):
                f_x(kind, 0).start()
                f_c(kind, 0, 0).start()
        for kind in (1, 0, 2):
            a_x_in(kind, order[step - 1]).wait_recv()
            a_c(kind, order[step - 1], 1).start()

    def hand_on(kind, step):
        for copy in f_z_in(kind, step):
            copy.wait_recv()
        f_x(kind, step).start()
        f_c(kind, step, 0).start()

    def cross(kind, step):
        f_x_in(kind, step).wait_recv()
        f_c(kind, step, 1).start()

    def pass_cotangent(step):
        d_z_in(order[step]).wait_recv()

        @pl.when(inner)
        def _():
            d_z(step).start()

        d_y(order[step]).start()

    for kind in (1, 0, 2):
        a_x_in(kind, order[z_size - 1]).wait_recv()
        a_c(kind, order[z_size - 1], 1).start()
    tok_y_in.wait_recv()
    own_q.wait()
    own_o.wait()
    for kind in (0, 1):
        for step in range(z_size):
            for far in range(2):
                a_c_in(kind, step, far).wait_recv()

    gains = kv_w[:, 2 * head :].astype(jnp.float32).T[:8, :]
    gain_ref[...] = gains

    def norm_rows(index, carry):
        at = pl.ds(pl.multiple_of(index * 32, 32), 32)
        values = tok[at, :].astype(jnp.float32)
        scale = lax.rsqrt(jnp.mean(values * values, axis=-1, keepdims=True) + epsilon)
        n1_ref[at, :] = (values * scale * gain_ref[0:1, :]).astype(jnp.bfloat16)
        return carry

    lax.fori_loop(0, 2 * own // 32, norm_rows, 0)
    hand_on(0, 1)
    table = (table_ref[0], table_ref[1])
    key_ref[...] = spin(dot_nn(n1_ref[...], kv_w[:, :head]), table).astype(jnp.bfloat16)
    val_ref[...] = dot_nn(n1_ref[...], kv_w[:, head : 2 * head]).astype(jnp.bfloat16)
    hand_on(0, 3)
    head_scale = head ** (-0.5)
    heads = att_ref.shape[1] // head

    half_cols = att_ref.shape[1] // 2
    for index in range(2):
        cols = pl.ds(index * half_cols, half_cols)
        query[:, cols] = dot_nn(n1_ref[...], q_w[:, cols])

    def attend(index):
        cols = pl.ds(index * head, head)
        rotated = (spin(query[:, cols], table) * head_scale).astype(jnp.bfloat16)
        rot_ref[:, cols] = rotated
        probs = head_probs(rotated, key_ref[...], allow_ref[...]).astype(jnp.bfloat16)
        att_ref[:, cols] = dot_nn(probs, val_ref[...]).astype(jnp.bfloat16)

    tasks = [
        lambda: hand_on(0, 2),
        lambda: pass_cotangent(1),
        lambda: hand_on(1, 1),
        lambda: cross(0, 0),
        lambda: hand_on(1, 3),
    ]
    for index in range(heads):
        attend(index)
        if index < len(tasks):
            tasks[index]()
    for step in range(z_size):
        for far in range(2):
            a_c_in(2, step, far).wait_recv()
    saves = [
        local(kv_w, kv_out),
        local(q_w, wq_out),
        local(o_w, wo_out),
    ]
    span = width // 4

    def project(index, carry):
        cols = pl.ds(pl.multiple_of(index * span, span), span)
        part[:, cols] = matmul_nt(att_ref[...], o_w[cols, :]).astype(jnp.bfloat16)
        return carry

    lax.fori_loop(0, 4, project, 0)
    part_out.start()
    hand_on(1, 2)
    cross(1, 0)
    cross(2, 0)
    cross(0, 1)
    pass_cotangent(2)
    hand_on(2, 1)
    part_out.wait_recv()

    def middle(index, carry):
        at = pl.ds(pl.multiple_of(index * 32, 32), 32)
        there = pl.ds(pl.multiple_of(me_y * own + index * 32, 32), 32)
        values = (
            tok_ref[at, :].astype(jnp.float32)
            + part[there, :].astype(jnp.float32)
            + part_y[at, :].astype(jnp.float32)
        )
        mid_ref[at, :] = values
        scale = lax.rsqrt(jnp.mean(values * values, axis=-1, keepdims=True) + epsilon)
        n2_ref[there, :] = (values * scale * gain_ref[1:2, :]).astype(jnp.bfloat16)
        return carry

    lax.fori_loop(0, own // 32, middle, 0)
    n2_y.start()
    hand_on(2, 3)
    cross(0, 3)
    pass_cotangent(3)
    hand_on(2, 2)
    cross(0, 2)
    for kind in (1, 2):
        for step in (1, 3, 2):
            cross(kind, step)
    for kind in range(3):
        for step in range(z_size):
            for far in range(2):
                f_c_in(kind, step, far).wait_recv()
    for step in range(z_size):
        d_y_in(step).wait_recv()
    n2_y_in.wait_recv()

    for kind in range(3):
        a_z_done(kind)
    d_z_done()
    kv_y.wait_send()
    tok_y.wait_send()
    part_out.wait_send()
    n2_y.wait_send()
    own_d.wait()
    for copy in saves:
        copy.wait()
    for step in range(z_size):
        d_y(step).wait_send()
        for kind in range(3):
            if step:
                for copy in f_z(kind, step):
                    copy.wait_send()
            a_x(kind, step).wait_send()
            f_x(kind, step).wait_send()
            for far in range(2):
                a_c(kind, step, far).wait_send()
                f_c(kind, step, far).wait_send()


def pre_call(tokens, kv_gains, table, allowed, cotangent, w_query, w_out, ffn):
    z_size = lax.axis_size("z")
    own, width = tokens.shape
    seq = 2 * own
    rows, cols = w_query.shape
    head = table.shape[2] * 2
    units = ragged_split(ffn[0].shape[1], z_size)[1]
    low = lambda *dims: jax.ShapeDtypeStruct(dims, jnp.bfloat16)
    full = lambda *dims: jax.ShapeDtypeStruct(dims, jnp.float32)
    dma = lambda *lead: pltpu.SemaphoreType.DMA(lead)
    vmem = pl.BlockSpec(memory_space=pltpu.VMEM)
    hbm = pl.BlockSpec(memory_space=pl.ANY)
    wide = lambda *lead: pltpu.VMEM((*lead, width), jnp.bfloat16)
    return pl.pallas_call(
        functools.partial(pre_kernel, z_size),
        out_shape=(
            low(seq, width),
            low(seq, cols),
            low(seq, head),
            low(seq, head),
            low(seq, cols),
            full(own, width),
            low(seq, width),
            full(8, width),
            low(width, kv_gains.shape[1]),
            low(width, cols),
            low(width, cols),
            low(3, width, units),
            low(z_size, seq, width),
        ),
        in_specs=[vmem] * 4 + [hbm] * 6,
        out_specs=(vmem,) * 8 + (hbm,) * 5,
        scratch_shapes=[
            pltpu.VMEM((width, kv_gains.shape[1]), jnp.bfloat16),
            pltpu.VMEM((width, cols), jnp.bfloat16),
            pltpu.VMEM((width, cols), jnp.bfloat16),
            wide(seq),
            wide(seq),
            wide(own),
            pltpu.VMEM((seq, cols), jnp.float32),
            dma(4),
            dma(4),
            dma(3, z_size + 1),
            dma(3, z_size),
            dma(3, z_size),
            dma(3, z_size),
            dma(3, 2 * z_size),
            dma(3, 2 * z_size),
            dma(3, z_size, 2),
            dma(3, z_size, 2),
            dma(3, z_size),
            dma(3, z_size),
            dma(3, 2 * z_size),
            dma(3, 2 * z_size),
            dma(z_size + 1),
            dma(z_size),
            dma(z_size),
            dma(z_size),
            dma(16),
        ],
        compiler_params=pltpu.CompilerParams(
            collective_id=1, has_side_effects=True, vmem_limit_bytes=VMEM_BYTES
        ),
        cost_estimate=pl.CostEstimate(
            flops=8 * seq * width * cols,
            bytes_accessed=8 * width * (cols + units),
            transcendentals=seq * seq * cols // head,
        ),
    )(tokens, kv_gains, table, allowed, cotangent, w_query, w_out, *ffn)


def norm_back(values, gain, upstream):
    scale = lax.rsqrt(jnp.mean(values * values, axis=-1, keepdims=True) + epsilon)
    normed = values * scale
    pulled = gain * upstream
    back = scale * (pulled - normed * jnp.mean(normed * pulled, axis=-1, keepdims=True))
    return back, jnp.sum(upstream * normed, axis=0, keepdims=True)


def post_kernel(
    z_size,
    mid_ref,
    tok_ref,
    cot_ref,
    gain_ref,
    n1_ref,
    rot_ref,
    key_ref,
    val_ref,
    att_ref,
    table_ref,
    allow_ref,
    kv_hbm,
    wq_hbm,
    wo_hbm,
    mix_hbm,
    gn_hbm,
    sums_hbm,
    mixed_ref,
    tgrad_ref,
    gsum_ref,
    kvg_ref,
    qg_ref,
    og_ref,
    ffn_out,
    kv_w,
    q_w,
    o_w,
    o_part,
    gm,
    gm_f,
    gq,
    gkv,
    kv_sum,
    back_y,
    mix_y,
    mix_z,
    mix_s,
    o_c,
    o_x,
    o_z,
    q_c,
    q_x,
    q_z,
    kv_y,
    kv_c,
    kv_x,
    kv_z,
    gain_own,
    gain_in,
    ffn_in,
    ffn_own,
    load_sem,
    own_sem,
    fx_send,
    fx_recv,
    fz_send,
    fz_recv,
    y_send,
    y_recv,
    my_send,
    my_recv,
    mz_send,
    mz_recv,
    wc_send,
    wc_recv,
    wx_send,
    wx_recv,
    wz_send,
    wz_recv,
    kc_send,
    kc_recv,
    kz_send,
    kz_recv,
    g_send,
    g_recv,
):
    me_z, me_x = lax.axis_index("z"), lax.axis_index("x")
    me_c, me_y = lax.axis_index("c"), lax.axis_index("mp")
    own, width = tok_ref.shape
    seq = 2 * own
    head = key_ref.shape[1]
    cols_here = att_ref.shape[1]
    heads = cols_here // head
    rows = qg_ref.shape[0]
    span = width // z_size
    mine = pl.ds(pl.multiple_of(me_y * own, own), own)
    theirs = pl.ds(pl.multiple_of((1 - me_y) * own, own), own)
    to_y, to_x, to_c = {"mp": 1 - me_y}, {"x": 1 - me_x}, {"c": 1 - me_c}
    head_scale = head ** (-0.5)

    def behind(step):
        return lax.rem(me_z - step + z_size, z_size)

    def to_z(step):
        return {"z": lax.rem(me_z + step, z_size)}

    def row_block(step, x_at, c_at):
        start = ((behind(step) * 2 + x_at) * 2 + c_at) * rows
        return pl.ds(pl.multiple_of(start, rows), rows)

    loads = [
        pltpu.make_async_copy(wo_hbm, o_w, load_sem.at[0]),
        pltpu.make_async_copy(wq_hbm, q_w, load_sem.at[1]),
        pltpu.make_async_copy(
            kv_hbm.at[:, :, :, :, :, pl.ds(0, 2 * head)], kv_w, load_sem.at[2]
        ),
    ]
    for step in range(z_size):
        loads.append(
            pltpu.make_async_copy(mix_hbm.at[step, me_y], mix_s.at[step], load_sem.at[3 + step])
        )
    gn_load = pltpu.make_async_copy(gn_hbm, gm_f, load_sem.at[3 + z_size])
    gn_load.start()
    for load in loads:
        load.start()

    barrier = pltpu.get_barrier_semaphore()
    peers = [to_y, to_x, to_c] + [to_z(step) for step in range(1, z_size)]
    for where in peers:
        pl.semaphore_signal(barrier, inc=1, device_id=where, device_id_type=MESH_ID)
    pl.semaphore_wait(barrier, len(peers))

    tasks = [(step, kind) for step in (2, 3) for kind in range(3)]

    def f_x(index):
        step, kind = tasks[index]
        return remote(
            sums_hbm.at[kind, step, 1],
            ffn_in.at[index],
            fx_send.at[index],
            fx_recv.at[index],
            to_x,
        )

    def f_own(index):
        step, kind = tasks[index]
        return pltpu.make_async_copy(
            sums_hbm.at[kind, step, 0], ffn_own.at[index % 2], own_sem.at[index % 2]
        )

    def f_z(step, kind):
        if step == 1:
            src = sums_hbm.at[kind, 1, 0]
        else:
            src = ffn_in.at[tasks.index((step, kind))]
        return remote(
            src, ffn_out.at[kind, step], fz_send.at[kind, step], fz_recv.at[kind, step], to_z(step)
        )

    def tick(index):
        step, kind = tasks[index]
        f_x(index).wait_recv()
        f_own(index).wait()
        block = ffn_in.at[index]
        add_rows(block, [ffn_own.at[index % 2]], block, rows)
        if index + 2 < len(tasks):
            f_own(index + 2).start()
        f_z(step, kind).start()

    def f_x_own(kind):
        return remote(
            sums_hbm.at[kind, 0, 1],
            ffn_out.at[kind, 0],
            fx_send.at[len(tasks) + kind],
            fx_recv.at[len(tasks) + kind],
            to_x,
        )

    f_own(0).start()
    f_own(1).start()
    for index in range(len(tasks)):
        f_x(index).start()
    for kind in range(3):
        f_z(1, kind).start()

    gn_load.wait()

    def mid_rows(index, total):
        at = pl.ds(pl.multiple_of(index * 32, 32), 32)
        grad, gain_part = norm_back(mid_ref[at, :], gain_ref[1:2, :], gm_f[at, :])
        grad = grad + cot_ref[at, :].astype(jnp.float32)
        gm_f[at, :] = grad
        gm[pl.ds(pl.multiple_of(me_y * own + index * 32, 32), 32), :] = grad.astype(jnp.bfloat16)
        return total + gain_part

    ffn_gain_part = lax.fori_loop(
        0, own // 32, mid_rows, jnp.zeros((1, width), jnp.float32)
    )
    gm_y = remote(gm.at[mine], gm.at[mine], y_send.at[0], y_recv.at[0], to_y)
    gm_y_in = remote(gm.at[theirs], gm.at[theirs], y_send.at[0], y_recv.at[0], to_y)
    gm_y.start()

    def mix_over_y(step):
        return remote(
            mix_hbm.at[step, 1 - me_y], mix_y.at[step], my_send.at[step], my_recv.at[step], to_y
        )

    def mix_over_z(step):
        return remote(
            mix_s.at[step], mix_z.at[step - 1], mz_send.at[step], mz_recv.at[step - 1], to_z(1)
        )

    def mix_step(step):
        mix_over_y(step).wait_recv()
        slot = (step - 2) % z_size
        others = [mix_y.at[step]]
        if step != 1:
            remote(
                mix_s.at[1], mix_z.at[slot], mz_send.at[1], mz_recv.at[slot], to_z(1)
            ).wait_recv()
            others.append(mix_z.at[slot])
        if step:
            def add_tile(tile, carry):
                at = pl.ds(pl.multiple_of(tile * TILE, TILE), TILE)
                total = mix_s[step, at, :].astype(jnp.float32)
                for other in others:
                    total = total + other[at, :].astype(jnp.float32)
                mix_s[step, at, :] = total.astype(jnp.bfloat16)
                return carry

            lax.fori_loop(0, width // TILE, add_tile, 0)
            mix_over_z(step).start()
        else:
            def last_tile(tile, carry):
                at = pl.ds(pl.multiple_of(tile * TILE, TILE), TILE)
                total = mix_s[0, at, :].astype(jnp.float32)
                for other in others:
                    total = total + other[at, :].astype(jnp.float32)
                mixed_ref[:, at] = (mid_ref[:, at] + total.T).astype(jnp.bfloat16)
                return carry

            lax.fori_loop(0, width // TILE, last_tile, 0)

    for step in (1, 2, 3, 0):
        mix_over_y(step).start()

    kinds = ((o_part, o_c, o_x, o_z, og_ref), (o_w, q_c, q_x, q_z, qg_ref))

    def w_c(kind, step, far):
        x_at = 1 - me_x if far else me_x
        return remote(
            kinds[kind][0].at[row_block(step, x_at, 1 - me_c)],
            kinds[kind][1].at[step, far],
            wc_send.at[kind, step, far],
            wc_recv.at[kind, step, far],
            to_c,
        )

    def w_x(kind, step):
        return remote(
            kinds[kind][0].at[row_block(step, 1 - me_x, me_c)],
            kinds[kind][2].at[step],
            wx_send.at[kind, step],
            wx_recv.at[kind, step],
            to_x,
        )

    first_z, last_z = (z_size - 1 - me_z) // (z_size - 1), me_z // (z_size - 1)
    inner = first_z + last_z == 0
    order = (
        0,
        1 + (me_z + 1) // 2,
        2 + (2 * me_z - 3) * (1 - first_z - last_z),
        3 - 2 * (me_z // 2),
    )
    right = (None, 1 - me_z // 2, (3 - me_z) * (2 - me_z) // 6 + me_z // 2 * (1 - last_z), 1 - me_z // 2)

    def w_z(kind, index):
        step, way = order[index], right[index]
        slot = way * lax.rem(step + 1, z_size) + (1 - way) * (step - 1 + 4 * ((3 - step) // 2))
        return remote(
            kinds[kind][0].at[row_block(step, me_x, me_c)],
            kinds[kind][3].at[slot],
            wz_send.at[kind, index],
            wz_recv.at[kind, slot],
            {"z": me_z + 2 * way - 1},
        )

    def w_z_in(kind, slot):
        block = kinds[kind][3].at[slot]
        return remote(block, block, wz_send.at[kind, 1], wz_recv.at[kind, slot], to_z(1))

    def w_x_stage(kind, index):
        step = order[index]
        w_c(kind, step, 1).wait_recv()
        block = kinds[kind][0].at[row_block(step, 1 - me_x, me_c)]
        add_rows(block, [kinds[kind][1].at[step, 1]], block, rows)
        w_x(kind, step).start()

    def w_z_stage(kind, index):
        part, from_c, from_x, from_z, result = kinds[kind]
        step = order[index]
        w_c(kind, step, 0).wait_recv()
        w_x(kind, step).wait_recv()
        block = part.at[row_block(step, me_x, me_c)]
        others = [from_c.at[step, 0], from_x.at[step]]
        if index:

            @pl.when(inner)
            def _():
                w_z_in(kind, step).wait_recv()
                add_rows(block, [*others, from_z.at[step]], block, rows)

            @pl.when(first_z + last_z > 0)
            def _():
                add_rows(block, others, block, rows)

            w_z(kind, index).start()
        else:

            @pl.when(first_z == 0)
            def _():
                w_z_in(kind, 0).wait_recv()

            @pl.when(last_z == 0)
            def _():
                w_z_in(kind, z_size).wait_recv()

            @pl.when(inner)
            def _():
                add_rows(block, [*others, from_z.at[0], from_z.at[z_size]], result, rows)

            @pl.when(first_z > 0)
            def _():
                add_rows(block, [*others, from_z.at[z_size]], result, rows)

            @pl.when(last_z > 0)
            def _():
                add_rows(block, [*others, from_z.at[0]], result, rows)

    def w_product(kind, index, left, values):
        step = order[index]
        at = pl.ds(pl.multiple_of(behind(step) * span, 128), span)
        turned = left[:, at].T

        def tile_body(tile, carry):
            cols = pl.ds(pl.multiple_of(tile * TILE, TILE), TILE)
            kinds[kind][0][at, cols] = dot_nn(turned, values[:, cols]).astype(jnp.bfloat16)
            return carry

        lax.fori_loop(0, cols_here // TILE, tile_body, 0)
        for far in (1, 0):
            w_c(kind, step, far).start()

    tick(0)
    tick(1)
    gm_y_in.wait_recv()
    w_product(0, 1, gm, att_ref)
    w_product(0, 2, gm, att_ref)
    w_x_stage(0, 1)
    w_product(0, 3, gm, att_ref)
    w_x_stage(0, 2)
    tick(2)
    w_product(0, 0, gm, att_ref)
    w_x_stage(0, 3)
    for load in loads:
        load.wait()

    kv_sum[...] = jnp.zeros(kv_sum.shape, jnp.float32)
    table = (table_ref[0], table_ref[1])

    for index in range(2):
        cols = pl.ds(index * (cols_here // 2), cols_here // 2)
        gq[:, cols] = dot_nn(gm[...], o_w[:, cols]).astype(jnp.bfloat16)

    def attend_back(index):
        cols = pl.ds(index * head, head)
        grad_vals = gq[:, cols]
        rotated = rot_ref[:, cols]
        probs = head_probs(rotated, key_ref[...], allow_ref[...])
        grad_probs = matmul_nt(grad_vals, val_ref[...])
        delta = jnp.sum(probs * grad_probs, axis=-1, keepdims=True)
        grad_scores = (probs * (grad_probs - delta)).astype(jnp.bfloat16)
        grad_rot = dot_nn(grad_scores, key_ref[...])
        gq[:, cols] = (spin_back(grad_rot, table) * head_scale).astype(jnp.bfloat16)
        kv_sum[0] += matmul_tn(grad_scores, rotated)
        kv_sum[1] += matmul_tn(probs.astype(jnp.bfloat16), grad_vals)

    for index in range(heads):
        attend_back(index)
        if index == 0:
            w_x_stage(0, 0)
        if 3 + index < len(tasks):
            tick(3 + index)
    gkv[:, :head] = spin_back(kv_sum[0], table).astype(jnp.bfloat16)
    gkv[:, head:] = kv_sum[1].astype(jnp.bfloat16)

    w_product(1, 1, n1_ref, gq)
    mix_step(1)
    w_product(1, 2, n1_ref, gq)
    w_x_stage(1, 1)
    w_z_stage(0, 1)
    w_product(1, 3, n1_ref, gq)
    w_x_stage(1, 2)
    w_product(1, 0, n1_ref, gq)
    w_x_stage(1, 3)
    w_x_stage(1, 0)
    for kind in range(3):
        f_x_own(kind).start()
    mix_step(2)

    gm_y.wait_send()
    back = gm
    def input_tile(index, carry):
        at = pl.ds(pl.multiple_of(index * span, 128), span)
        back[:, at] = (
            matmul_nt(gq[...], q_w[at, :]) + matmul_nt(gkv[...], kv_w[index].reshape(span, 2 * head))
        ).astype(jnp.bfloat16)
        return carry

    lax.fori_loop(0, z_size, input_tile, 0)
    back_out = remote(back.at[theirs], back_y, y_send.at[1], y_recv.at[1], to_y)
    back_out.start()

    kv_part = kv_w

    def kv_tile(index, carry):
        at = pl.ds(pl.multiple_of(index * span, 128), span)
        product = dot_nn(n1_ref[:, at].T, gkv[...]).astype(jnp.bfloat16)
        kv_part[index] = product.reshape(kv_part.shape[1:])
        return carry

    lax.fori_loop(0, z_size, kv_tile, 0)
    kv_over_y = remote(kv_part.at[:, :, :, 1 - me_y], kv_y, y_send.at[2], y_recv.at[2], to_y)
    kv_over_y.start()
    w_z_stage(0, 2)
    mix_step(3)
    kv_over_y.wait_recv()

    def kv_add_y(index, carry):
        for x_at in range(2):
            for c_at in range(2):
                block = kv_part.at[index, x_at, c_at, me_y]
                block[...] = (
                    block[...].astype(jnp.float32) + kv_y[index, x_at, c_at].astype(jnp.float32)
                ).astype(jnp.bfloat16)
        return carry

    lax.fori_loop(0, z_size, kv_add_y, 0)
    kv_over_c = remote(
        kv_part.at[:, :, 1 - me_c, me_y], kv_c, kc_send.at[0], kc_recv.at[0], to_c
    )
    kv_over_c.start()
    w_z_stage(0, 3)
    w_z_stage(1, 1)
    kv_over_c.wait_recv()

    def kv_add_c(index, carry):
        for x_at in range(2):
            block = kv_part.at[index, x_at, me_c, me_y]
            block[...] = (
                block[...].astype(jnp.float32) + kv_c[index, x_at].astype(jnp.float32)
            ).astype(jnp.bfloat16)
        return carry

    lax.fori_loop(0, z_size, kv_add_c, 0)
    kv_over_x = remote(
        kv_part.at[:, 1 - me_x, me_c, me_y], kv_x, kc_send.at[1], kc_recv.at[1], to_x
    )
    kv_over_x.start()

    back_out.wait_recv()

    def input_rows(index, total):
        at = pl.ds(pl.multiple_of(index * 32, 32), 32)
        there = pl.ds(pl.multiple_of(me_y * own + index * 32, 32), 32)
        upstream = back[there, :].astype(jnp.float32) + back_y[at, :].astype(jnp.float32)
        grad, gain_part = norm_back(
            tok_ref[at, :].astype(jnp.float32), gain_ref[0:1, :], upstream
        )
        tgrad_ref[at, :] = (gm_f[at, :] + grad).astype(jnp.bfloat16)
        return total + gain_part

    attn_gain_part = lax.fori_loop(
        0, own // 32, input_rows, jnp.zeros((1, width), jnp.float32)
    )
    for index in range(4):
        at = slice(index * span, (index + 1) * span)
        gain_own[0, index : index + 1, :] = attn_gain_part[:, at]
        gain_own[0, 4 + index : 5 + index, :] = ffn_gain_part[:, at]

    def gain_send(stage, where):
        return remote(
            gain_own.at[stage], gain_in.at[stage], g_send.at[stage], g_recv.at[stage], where
        )

    gain_hops = [gain_send(0, to_y), gain_send(1, to_c), gain_send(2, to_x)]
    gain_last = [
        remote(
            gain_own.at[3], gain_in.at[2 + step], g_send.at[2 + step], g_recv.at[2 + step], to_z(step)
        )
        for step in range(1, z_size)
    ]

    def gain_fold(stage):
        gain_hops[stage].wait_recv()
        gain_own[stage + 1] = gain_own[stage] + gain_in[stage]

    gain_hops[0].start()
    mix_step(0)
    w_z_stage(0, 0)
    gain_fold(0)
    gain_hops[1].start()
    w_z_stage(1, 2)
    gain_fold(1)
    gain_hops[2].start()
    gain_fold(2)
    for copy in gain_last:
        copy.start()

    kv_over_x.wait_recv()

    def kv_add_x(index, carry):
        block = kv_part.at[index, me_x, me_c, me_y]
        block[...] = (
            block[...].astype(jnp.float32) + kv_x[index].astype(jnp.float32)
        ).astype(jnp.bfloat16)
        return carry

    lax.fori_loop(0, z_size, kv_add_x, 0)
    kv_over_z = [
        remote(
            kv_part.at[lax.rem(me_z + step, z_size), me_x, me_c, me_y],
            kv_z.at[step - 1],
            kz_send.at[step],
            kz_recv.at[step],
            to_z(step),
        )
        for step in range(1, z_size)
    ]
    for copy in kv_over_z:
        copy.start()
    w_z_stage(1, 3)
    for copy in gain_last:
        copy.wait_recv()
    gsum_ref[...] = gain_own[3] + gain_in[3] + gain_in[4] + gain_in[5]
    for copy in kv_over_z:
        copy.wait_recv()
    kvg_ref[...] = (
        kv_part[me_z, me_x, me_c, me_y].astype(jnp.float32)
        + kv_z[0].astype(jnp.float32)
        + kv_z[1].astype(jnp.float32)
        + kv_z[2].astype(jnp.float32)
    )
    w_z_stage(1, 0)

    back_out.wait_send()
    kv_over_y.wait_send()
    kv_over_c.wait_send()
    kv_over_x.wait_send()
    for kind in range(3):
        f_x_own(kind).wait()
    for index in range(len(tasks)):
        f_x(index).wait_send()
    for step in range(1, z_size):
        for kind in range(3):
            f_z(step, kind).wait()
    for copy in gain_hops + gain_last + kv_over_z:
        copy.wait_send()
    for step in range(z_size):
        mix_over_y(step).wait_send()
        if step:
            mix_over_z(step).wait_send()
        for kind in range(2):
            w_c(kind, step, 0).wait_send()
            w_c(kind, step, 1).wait_send()
            w_x(kind, step).wait_send()
            if step:
                w_z(kind, step).wait_send()


def post_call(
    grad_normed,
    mid,
    tokens,
    cotangent,
    gains,
    normed_one,
    rotated,
    keys,
    values,
    attn_vals,
    table,
    allowed,
    kv_weight,
    query_weight,
    out_weight,
    mix_parts,
    ffn_sums,
):
    z_size = lax.axis_size("z")
    own, width = tokens.shape
    seq = 2 * own
    head = keys.shape[1]
    cols = attn_vals.shape[1]
    rows = width // (4 * z_size)
    units = ffn_sums.shape[4]
    low = lambda *dims: pltpu.VMEM(dims, jnp.bfloat16)
    full = lambda *dims: pltpu.VMEM(dims, jnp.float32)
    out_full = lambda *dims: jax.ShapeDtypeStruct(dims, jnp.float32)
    out_low = lambda *dims: jax.ShapeDtypeStruct(dims, jnp.bfloat16)
    dma = lambda *lead: pltpu.SemaphoreType.DMA(lead)
    vmem = pl.BlockSpec(memory_space=pltpu.VMEM)
    hbm = pl.BlockSpec(memory_space=pl.ANY)
    z = z_size
    return pl.pallas_call(
        functools.partial(post_kernel, z_size),
        out_shape=(
            out_low(own, width),
            out_low(own, width),
            out_full(8, width // z),
            out_full(rows // 2, 2 * head),
            out_full(rows, cols),
            out_full(rows, cols),
            out_low(3, z, rows, units),
        ),
        in_specs=[vmem] * 11 + [hbm] * 6,
        out_specs=(vmem,) * 6 + (hbm,),
        scratch_shapes=[
            low(z, 2, 2, 2, rows // 2, 2 * head),
            low(width, cols),
            low(width, cols),
            low(width, cols),
            low(seq, width),
            full(own, width),
            low(seq, cols),
            low(seq, 2 * head),
            full(2, seq, head),
            low(own, width),
            low(z, width, own),
            low(z - 1, width, own),
            low(z, width, own),
            low(z, 2, rows, cols),
            low(z, rows, cols),
            low(z + 1, rows, cols),
            low(z, 2, rows, cols),
            low(z, rows, cols),
            low(z + 1, rows, cols),
            low(z, 2, 2, rows // 2, 2 * head),
            low(z, 2, rows // 2, 2 * head),
            low(z, rows // 2, 2 * head),
            low(z - 1, rows // 2, 2 * head),
            full(4, 8, width // z),
            full(6, 8, width // z),
            low(6, rows, units),
            low(2, rows, units),
            dma(4 + z),
            dma(2),
            dma(9),
            dma(9),
            dma(3, z),
            dma(3, z),
            dma(3),
            dma(3),
            dma(z),
            dma(z),
            dma(z),
            dma(z),
            dma(2, z, 2),
            dma(2, z, 2),
            dma(2, z),
            dma(2, z),
            dma(2, z),
            dma(2, z + 1),
            dma(2),
            dma(2),
            dma(z),
            dma(z),
            dma(6),
            dma(6),
        ],
        compiler_params=pltpu.CompilerParams(
            collective_id=2, has_side_effects=True, vmem_limit_bytes=VMEM_BYTES
        ),
        cost_estimate=pl.CostEstimate(
            flops=14 * seq * width * cols,
            bytes_accessed=10 * width * cols,
            transcendentals=seq * seq * cols // head,
        ),
    )(
        mid,
        tokens,
        cotangent,
        gains,
        normed_one,
        rotated,
        keys,
        values,
        attn_vals,
        table,
        allowed,
        kv_weight.reshape(z, 2, 2, 2, rows // 2, kv_weight.shape[1]),
        query_weight,
        out_weight,
        mix_parts,
        grad_normed,
        ffn_sums,
    )


def layout_kernel(
    z_size, main, sum_ref, ffn_ref, q_ref, o_ref, kv_ref, wg_ref, wu_ref, wd_ref, qg_ref, og_ref, kvg_ref
):
    me_z = lax.axis_index("z")
    for kind, out in enumerate((wg_ref, wu_ref, wd_ref)):
        out[:, z_size * main :] = jnp.zeros((out.shape[0], 64 * z_size), jnp.float32)
        for step in range(z_size):
            at = lax.rem(me_z - step + z_size, z_size)
            values = ffn_ref[kind, step].astype(jnp.float32)
            if step == 0:
                values = values + sum_ref[kind, 0, 0].astype(jnp.float32)
            body = pl.ds(pl.multiple_of(at * main, 128), main)
            out[:, body] = values[:, :main]
            tail = pl.ds(pl.multiple_of(z_size * main + at // 2 * 128, 128), 128)
            out[:, tail] += values[:, main:]
    qg_ref[...] = q_ref[...]
    og_ref[...] = o_ref[...]
    kvg_ref[...] = kv_ref[...]


def layout_call(ffn_sums, ffn_grads, query_grad, out_grad, kv_grad, ffn_cols):
    z_size = lax.axis_size("z")
    main, units = ragged_split(ffn_cols, z_size)
    rows, cols = query_grad.shape
    parts = rows // 32
    kv_rows = kv_grad.shape[0] // parts
    full = lambda *dims: jax.ShapeDtypeStruct(dims, jnp.float32)
    row = lambda height, width: pl.BlockSpec((height, width), lambda index: (index, 0))
    specs = [row(32, cols), row(32, cols), row(kv_rows, kv_grad.shape[1])]
    return pl.pallas_call(
        functools.partial(layout_kernel, z_size, main),
        grid=(parts,),
        out_shape=(
            *[full(rows, ffn_cols)] * 3,
            full(rows, cols),
            full(rows, cols),
            full(*kv_grad.shape),
        ),
        in_specs=[
            pl.BlockSpec((3, 1, 1, 32, units), lambda index: (0, 0, 0, index, 0)),
            pl.BlockSpec((3, z_size, 32, units), lambda index: (0, 0, index, 0)),
            *specs,
        ],
        out_specs=(*[row(32, ffn_cols)] * 3, *specs),
        compiler_params=pltpu.CompilerParams(vmem_limit_bytes=32 * 1024 * 1024),
    )(ffn_sums, ffn_grads, query_grad, out_grad, kv_grad)


FF_SPLIT = 4


def ffn_pass(normed, grad_out, gate_weight, up_weight, down_weight):
    gate = jnp.dot(normed, gate_weight, preferred_element_type=jnp.float32)
    up_proj = jnp.dot(normed, up_weight, preferred_element_type=jnp.float32)
    grad_hidden = jnp.dot(grad_out, down_weight, preferred_element_type=jnp.float32)
    product, pull = jax.vjp(gelu_product, gate, up_proj)
    hidden = product.astype(jnp.bfloat16)
    grad_gate_f, grad_up_f = pull(grad_hidden)
    grad_gate = grad_gate_f.astype(jnp.bfloat16)
    grad_up = grad_up_f.astype(jnp.bfloat16)
    mixed_part = matmul_nt(hidden, down_weight).astype(jnp.bfloat16)
    normed_part = (matmul_nt(grad_gate, gate_weight) + matmul_nt(grad_up, up_weight)).astype(
        jnp.bfloat16
    )
    weight_parts = [
        matmul_tn(normed, grad_gate).astype(jnp.bfloat16),
        matmul_tn(normed, grad_up).astype(jnp.bfloat16),
        matmul_tn(grad_out, hidden).astype(jnp.bfloat16),
    ]
    return mixed_part, normed_part, weight_parts


def shards_general(
    tokens,
    segments,
    positions,
    cotangent,
    attn_gain,
    ffn_gain,
    w_kv,
    w_query,
    w_out,
    w_gate,
    w_up,
    w_down,
):
    everywhere = ("z", "xc", "mp")
    dp = ("z", "xc")
    z_size = lax.axis_size("z")
    xc_size = lax.axis_size("xc")
    gains = lax.all_gather(
        jnp.stack([attn_gain, ffn_gain], axis=1), everywhere, axis=0, tiled=True
    ).astype(jnp.float32)
    gain_one, gain_two = gains[:, 0], gains[:, 1]
    kv_weight = lax.all_gather(w_kv, everywhere, axis=0, tiled=True)
    head_dim = kv_weight.shape[1] // 2
    width = tokens.shape[1]
    seq_len = segments.shape[0]
    heads_here = w_query.shape[1] // head_dim
    scale = head_dim ** (-0.5)
    cosine, sine = rotary_angles(positions, head_dim)
    inputs_f = tokens.astype(jnp.float32)
    tokens_all = lax.all_gather(tokens, "mp", axis=0, tiled=True)
    normed_one = norm_gain(tokens_all.astype(jnp.float32), gain_one).astype(jnp.bfloat16)
    query_weight = lax.all_gather(w_query, dp, axis=0, tiled=True)
    out_weight = lax.all_gather(w_out, dp, axis=0, tiled=True)

    rows = w_gate.shape[0]
    unit = w_gate.shape[1] // z_size

    def spread(weight):
        pieces = weight.reshape(rows, z_size, unit).transpose(1, 0, 2)
        pieces = lax.all_to_all(pieces, "z", split_axis=0, concat_axis=0, tiled=True)
        return lax.all_gather(pieces, "xc", axis=1, tiled=False).reshape(width, unit)

    gate_weight, up_weight, down_weight = spread(w_gate), spread(w_up), spread(w_down)
    grad_all = lax.all_gather(cotangent, ("z", "mp"), axis=0, tiled=True)

    query = jnp.dot(normed_one, query_weight, preferred_element_type=jnp.float32).reshape(
        seq_len, heads_here, head_dim
    )
    rotated = (rotate(query, cosine[:, None], sine[:, None]) * scale).astype(jnp.bfloat16)
    keyval = jnp.dot(normed_one, kv_weight, preferred_element_type=jnp.float32)
    keys = rotate(keyval[:, :head_dim], cosine, sine).astype(jnp.bfloat16)
    values = keyval[:, head_dim:].astype(jnp.bfloat16)
    allowed = block_allowed(segments, 0, seq_len)
    scores = jnp.einsum("thd,sd->hts", rotated, keys, preferred_element_type=jnp.float32)
    scores = jnp.where(allowed[None], scores, masked_score)
    row_max = jnp.max(scores, axis=-1, keepdims=True)
    weights = jnp.exp(scores - row_max)
    probs = weights / jnp.sum(weights, axis=-1, keepdims=True)
    probs_low = probs.astype(jnp.bfloat16)
    attn_vals = (
        jnp.einsum("hts,sd->thd", probs_low, values, preferred_element_type=jnp.float32)
        .reshape(seq_len, heads_here * head_dim)
        .astype(jnp.bfloat16)
    )
    mid = inputs_f + lax.psum_scatter(
        matmul_nt(attn_vals, out_weight).astype(jnp.bfloat16),
        "mp",
        scatter_dimension=0,
        tiled=True,
    ).astype(jnp.float32)
    normed_two = norm_gain(mid, gain_two).astype(jnp.bfloat16)
    normed_all = lax.all_gather(normed_two, ("z", "mp"), axis=0, tiled=True)

    mixed_part, normed_part, weight_parts = ffn_pass(
        normed_all, grad_all, gate_weight, up_weight, down_weight
    )
    grad_normed_two = lax.psum_scatter(
        normed_part, ("z", "mp"), scatter_dimension=0, tiled=True
    ).astype(jnp.float32)
    mixed = (
        mid
        + lax.psum_scatter(mixed_part, ("z", "mp"), scatter_dimension=0, tiled=True).astype(
            jnp.float32
        )
    ).astype(jnp.bfloat16)

    def collect(part):
        pieces = part.reshape(z_size, xc_size, rows, unit).transpose(1, 0, 2, 3)
        pieces = pieces.reshape(xc_size * z_size * rows, unit)
        pieces = lax.psum_scatter(pieces, "xc", scatter_dimension=0, tiled=True)
        pieces = pieces.reshape(z_size, rows, unit)
        pieces = lax.all_to_all(pieces, "z", split_axis=0, concat_axis=0, tiled=True)
        return pieces.transpose(1, 0, 2).reshape(rows, z_size * unit).astype(jnp.float32)

    w_gate_grad, w_up_grad, w_down_grad = [collect(part) for part in weight_parts]

    norm_pull_two = jax.vjp(norm_gain, mid, gain_two)[1]
    grad_mid_norm, grad_gain_two = norm_pull_two(grad_normed_two)
    grad_mid = cotangent.astype(jnp.float32) + grad_mid_norm
    grad_mid_all = lax.all_gather(grad_mid.astype(jnp.bfloat16), "mp", axis=0, tiled=True)
    grad_vals = (
        jnp.dot(grad_mid_all, out_weight, preferred_element_type=jnp.float32)
        .astype(jnp.bfloat16)
        .reshape(seq_len, heads_here, head_dim)
    )
    grad_probs = jnp.einsum("thd,sd->hts", grad_vals, values, preferred_element_type=jnp.float32)
    delta = jnp.sum(probs * grad_probs, axis=-1, keepdims=True)
    grad_scores = (probs * (grad_probs - delta)).astype(jnp.bfloat16)
    grad_rot = jnp.einsum("hts,sd->thd", grad_scores, keys, preferred_element_type=jnp.float32)
    key_sum = jnp.einsum("hts,thd->sd", grad_scores, rotated, preferred_element_type=jnp.float32)
    value_sum = jnp.einsum("hts,thd->sd", probs_low, grad_vals, preferred_element_type=jnp.float32)
    grad_query = (
        (unrotate(grad_rot, cosine[:, None], sine[:, None]) * scale)
        .reshape(seq_len, heads_here * head_dim)
        .astype(jnp.bfloat16)
    )
    grad_kv = jnp.concatenate([unrotate(key_sum, cosine, sine), value_sum], axis=1).astype(
        jnp.bfloat16
    )
    grad_normed_one = lax.psum_scatter(
        (matmul_nt(grad_query, query_weight) + matmul_nt(grad_kv, kv_weight)).astype(jnp.bfloat16),
        "mp",
        scatter_dimension=0,
        tiled=True,
    ).astype(jnp.float32)
    norm_pull_one = jax.vjp(norm_gain, inputs_f, gain_one)[1]
    grad_input_norm, grad_gain_one = norm_pull_one(grad_normed_one)
    tokens_grad = (grad_mid + grad_input_norm).astype(jnp.bfloat16)

    w_query_grad = lax.psum_scatter(
        matmul_tn(normed_one, grad_query).astype(jnp.bfloat16), dp, scatter_dimension=0, tiled=True
    ).astype(jnp.float32)
    w_out_grad = lax.psum_scatter(
        matmul_tn(grad_mid_all, attn_vals).astype(jnp.bfloat16), dp, scatter_dimension=0, tiled=True
    ).astype(jnp.float32)
    small = jnp.concatenate(
        [matmul_tn(normed_one, grad_kv), grad_gain_one[:, None], grad_gain_two[:, None]], axis=1
    )
    small = lax.psum_scatter(small, everywhere, scatter_dimension=0, tiled=True)
    kv_grad = small[:, : 2 * head_dim]
    return (
        mixed,
        tokens_grad,
        small[:, 2 * head_dim],
        small[:, 2 * head_dim + 1],
        kv_grad,
        w_query_grad,
        w_out_grad,
        w_gate_grad,
        w_up_grad,
        w_down_grad,
    )


def shards_fast(
    tokens,
    segments,
    positions,
    cotangent,
    attn_gain,
    ffn_gain,
    w_kv,
    w_query,
    w_out,
    w_gate,
    w_up,
    w_down,
):
    seq_len = segments.shape[0]
    cosine, sine = rotary_angles(positions, w_kv.shape[1] // 2)
    table = jnp.stack(
        [
            jnp.concatenate([cosine, cosine], axis=1),
            jnp.concatenate([-sine, sine], axis=1),
        ]
    )
    allowed = block_allowed(segments, 0, seq_len).astype(jnp.float32)
    kv_gains = jnp.concatenate(
        [w_kv, attn_gain[:, None], ffn_gain[:, None], jnp.zeros((w_kv.shape[0], 126), w_kv.dtype)],
        axis=1,
    )
    (
        normed_one,
        rotated,
        keys,
        values,
        attn_vals,
        mid,
        normed_two,
        gains,
        kv_weight,
        query_weight,
        out_weight,
        ffn_weights,
        grad_all,
    ) = pre_call(
        tokens, kv_gains, table, allowed, cotangent, w_query, w_out, (w_gate, w_up, w_down)
    )
    main = ragged_split(w_gate.shape[1], lax.axis_size("z"))[0]
    grad_normed_two, mix_parts, ffn_sums = ffn_call(
        normed_two, grad_all, ffn_weights, w_gate.shape[0], main
    )
    mixed, tokens_grad, gain_grads, kv_grad, query_grad, out_grad, ffn_grads = post_call(
        grad_normed_two,
        mid,
        tokens,
        cotangent,
        gains,
        normed_one,
        rotated,
        keys,
        values,
        attn_vals,
        table,
        allowed,
        kv_weight,
        query_weight,
        out_weight,
        mix_parts,
        ffn_sums,
    )
    *ffn_out, query_grad, out_grad, kv_grad = layout_call(
        ffn_sums, ffn_grads, query_grad, out_grad, kv_grad, w_gate.shape[1]
    )
    share = attn_gain.shape[0]
    place = lax.axis_index(("z", "x", "c", "mp")) * share
    gain_grads = gain_grads.reshape(2, gain_grads.size // 2)
    gain_grads = lax.dynamic_slice(gain_grads, (0, place), (2, share))
    return (
        mixed,
        tokens_grad,
        gain_grads[0],
        gain_grads[1],
        kv_grad,
        query_grad,
        out_grad,
        *ffn_out,
    )


def solution(mesh):
    dp_size, mp_size = mesh.shape["dp"], mesh.shape["mp"]
    if dp_size == 4 * FF_SPLIT and mp_size == 2:
        body, dp = shards_fast, ("z", "x", "c")
        sizes = (FF_SPLIT, 2, 2, mp_size)
    else:
        body, dp = shards_general, ("z", "xc")
        sizes = (FF_SPLIT, dp_size // FF_SPLIT, mp_size)
    all_axes = (*dp, "mp")
    fine = jax.sharding.Mesh(mesh.devices.reshape(sizes), all_axes)
    in_specs = (
        P(all_axes, None),
        P(dp),
        P(dp),
        P(all_axes, None),
        P(all_axes),
        P(all_axes),
        P(all_axes, None),
        P(dp, "mp"),
        P(dp, "mp"),
        P(dp, "mp"),
        P(dp, "mp"),
        P(dp, "mp"),
    )
    out_specs = (
        P(all_axes, None),
        P(all_axes, None),
        P(all_axes),
        P(all_axes),
        P(all_axes, None),
        P(dp, "mp"),
        P(dp, "mp"),
        P(dp, "mp"),
        P(dp, "mp"),
        P(dp, "mp"),
    )
    return jax.shard_map(body, mesh=fine, in_specs=in_specs, out_specs=out_specs, check_vma=False)
```

```python
import functools

import jax
import jax.numpy as jnp
from jax import lax
from jax.experimental import pallas as pl
from jax.experimental.pallas import tpu as pltpu
from jax.sharding import PartitionSpec as P

WINDOW = 2048


epsilon = 1e-06
rope_base = 10000.0
masked_score = -1e30
VMEM_BYTES = 66_000_000


def norm_gain(values, gain):
    return values * lax.rsqrt(jnp.mean(values * values, axis=-1, keepdims=True) + epsilon) * gain


def rotary_angles(positions, head_width):
    quarter = head_width // 4
    freqs = rope_base ** (-jnp.arange(quarter).astype(jnp.float32) / quarter)
    phase = positions.astype(jnp.float32)[:, None] * freqs[None, :]
    return (jnp.cos(phase), jnp.sin(phase))


def rotate(values, cosine, sine):
    quarter = cosine.shape[-1]
    first_half = values[..., :quarter]
    second_half = values[..., quarter : 2 * quarter]
    return jnp.concatenate(
        [
            first_half * cosine - second_half * sine,
            second_half * cosine + first_half * sine,
            values[..., 2 * quarter :],
        ],
        axis=-1,
    )


def unrotate(values, cosine, sine):
    quarter = cosine.shape[-1]
    first_half = values[..., :quarter]
    second_half = values[..., quarter : 2 * quarter]
    return jnp.concatenate(
        [
            first_half * cosine + second_half * sine,
            second_half * cosine - first_half * sine,
            values[..., 2 * quarter :],
        ],
        axis=-1,
    )


def gelu_product(gate, up_proj):
    return jax.nn.gelu(gate, approximate=True) * up_proj


def matmul_nt(left, right):
    return lax.dot_general(
        left, right, (((1,), (1,)), ((), ())), preferred_element_type=jnp.float32
    )


def matmul_tn(left, right):
    return lax.dot_general(
        left, right, (((0,), (0,)), ((), ())), preferred_element_type=jnp.float32
    )


def block_allowed(segments, first_row, rows):
    seq_len = segments.shape[0]
    query_rows = first_row + jnp.arange(rows)
    key_rows = jnp.arange(seq_len)
    return (
        (segments[:, None] == segments[None, :])
        & (key_rows[None, :] <= query_rows[:, None])
        & (query_rows[:, None] - key_rows[None, :] < WINDOW)
    )


MESH_ID = pl.DeviceIdType.MESH
GELU_A = 0.7978845608028654
GELU_B = 0.044715
TILE = 256
WIDE = 512


def remote(src, dst, send_sem, recv_sem, where):
    return pltpu.make_async_remote_copy(
        src_ref=src,
        dst_ref=dst,
        send_sem=send_sem,
        recv_sem=recv_sem,
        device_id=where,
        device_id_type=MESH_ID,
    )


def dot_nn(left, right):
    return lax.dot_general(
        left, right, (((1,), (0,)), ((), ())), preferred_element_type=jnp.float32
    )


def gelu_parts(gate):
    square = gate * gate
    bend = jnp.tanh(GELU_A * gate * (1.0 + GELU_B * square))
    half = 0.5 * (1.0 + bend)
    slope = half + 0.5 * gate * (1.0 - bend * bend) * GELU_A * (1.0 + 3.0 * GELU_B * square)
    return gate * half, slope


def add_rows(first, rest, out, count):
    def body(index, carry):
        step = pl.ds(pl.multiple_of(index * 32, 32), 32)
        total = first[step, :].astype(jnp.float32)
        for other in rest:
            total = total + other[step, :].astype(jnp.float32)
        out[step, :] = total.astype(out.dtype)
        return carry

    lax.fori_loop(0, count // 32, body, 0)


def ffn_kernel(
    z_size,
    main,
    own_hbm,
    dy_hbm,
    w_hbm,
    gn_ref,
    mix_hbm,
    sums_hbm,
    n2,
    dy,
    w3,
    h3,
    n2_t,
    dy_t,
    gn_part,
    mix_buf,
    gn_y,
    gn_z,
    gn_s,
    c_in,
    x_in,
    load_sem,
    mix_sem,
    ag_y_send,
    ag_y_recv,
    ag_z_send,
    ag_z_recv,
    rs_y_send,
    rs_y_recv,
    rs_z_send,
    rs_z_recv,
    c_send,
    c_recv,
    x_send,
    x_recv,
    out_sem,
):
    own = own_hbm.shape[0] // 2
    width = own_hbm.shape[1]
    units = w3.shape[2]
    rows = c_in.shape[3]
    span = width // z_size
    me_y, me_z = lax.axis_index("mp"), lax.axis_index("z")
    me_x, me_c = lax.axis_index("x"), lax.axis_index("c")
    mine = pl.ds(pl.multiple_of(me_y * own, own), own)
    theirs = pl.ds(pl.multiple_of((1 - me_y) * own, own), own)
    to_y, to_x, to_c = {"mp": 1 - me_y}, {"x": 1 - me_x}, {"c": 1 - me_c}

    def ahead(step):
        return lax.rem(me_z + step, z_size)

    def to_z(step):
        return {"z": ahead(step)}

    def row_block(z_at, x_at, c_at):
        return pl.ds(pl.multiple_of(((z_at * 2 + x_at) * 2 + c_at) * rows, rows), rows)

    loads = []
    for index in range(3):
        loads.append(
            pltpu.make_async_copy(w_hbm.at[index], w3.at[index], load_sem.at[z_size + index])
        )
    dy_loads = [
        pltpu.make_async_copy(dy_hbm.at[index], dy, load_sem.at[index])
        for index in range(z_size)
    ]
    own_load = pltpu.make_async_copy(own_hbm, n2.at[0], load_sem.at[z_size + 3])
    for load in [own_load, dy_loads[0], *loads]:
        load.start()

    barrier = pltpu.get_barrier_semaphore()
    peers = [to_y, to_x, to_c] + [to_z(step) for step in range(1, z_size)]
    for where in peers:
        pl.semaphore_signal(barrier, inc=1, device_id=where, device_id_type=MESH_ID)
    pl.semaphore_wait(barrier, len(peers))

    def ag_y(index):
        block = n2.at[index, mine]
        return remote(block, block, ag_y_send.at[index], ag_y_recv.at[index], to_y)

    def ag_y_in(index):
        block = n2.at[index, theirs]
        return remote(block, block, ag_y_send.at[index], ag_y_recv.at[index], to_y)

    def ag_z(index):
        src = own_hbm.at[mine] if index == 0 else n2.at[index, mine]
        return remote(
            src, n2.at[index + 1, mine], ag_z_send.at[index], ag_z_recv.at[index + 1], to_z(1)
        )

    def ag_z_in(index):
        block = n2.at[index, mine]
        return remote(block, block, ag_z_send.at[0], ag_z_recv.at[index], to_z(1))

    def forward(index):
        ag_z_in(index).wait_recv()
        if index < z_size - 1:
            ag_z(index).start()
        ag_y(index).start()

    ag_z(0).start()

    mix_copies = []

    def turn(source, target, index):
        def turn_tile(tile, carry):
            at = pl.ds(pl.multiple_of(tile * span, 128), span)
            target[at, pl.ds(index * 2 * own, 2 * own)] = source[:, at].T
            return carry

        lax.fori_loop(0, z_size, turn_tile, 0)

    def chunk(index):
        if index:
            ag_y_in(index).wait_recv()
            mix_copies[index - 1].wait()
        else:
            own_load.wait()
        dy_loads[index].wait()
        rows_at = pl.ds(index * 2 * own, 2 * own)

        def up_tile(tile, carry):
            cols = pl.ds(pl.multiple_of(tile * TILE, TILE), TILE)
            gate = dot_nn(n2[index], w3[0, :, cols])
            up_proj = dot_nn(n2[index], w3[1, :, cols])
            grad_hidden = dot_nn(dy[...], w3[2, :, cols])
            act, slope = gelu_parts(gate)
            at = lax.broadcasted_iota(jnp.int32, (1, TILE), 1) + tile * TILE
            low_at = main + 64 * lax.rem(me_z, 2)
            keep = (at < main) | ((at >= low_at) & (at < low_at + 64))
            act = jnp.where(keep, act, 0.0)
            slope = jnp.where(keep, slope, 0.0)
            h3[0, rows_at, cols] = (grad_hidden * up_proj * slope).astype(jnp.bfloat16)
            h3[1, rows_at, cols] = (grad_hidden * act).astype(jnp.bfloat16)
            h3[2, rows_at, cols] = (act * up_proj).astype(jnp.bfloat16)
            return carry

        lax.fori_loop(0, units // TILE, up_tile, 0)

        def down_tile(tile, carry):
            at = pl.ds(pl.multiple_of(tile * span, 128), span)
            normed = matmul_nt(w3[0, at, :], h3[0, rows_at, :]) + matmul_nt(
                w3[1, at, :], h3[1, rows_at, :]
            )
            mixed = matmul_nt(w3[2, at, :], h3[2, rows_at, :])
            for half in range(2):
                cols = slice(half * own, (half + 1) * own)
                gn_part[index, half, at, :] = normed[:, cols].astype(jnp.bfloat16)
                mix_buf[half, at, :] = mixed[:, cols].astype(jnp.bfloat16)
            return carry

        lax.fori_loop(0, z_size, down_tile, 0)
        copy = pltpu.make_async_copy(mix_buf, mix_hbm.at[index], mix_sem.at[index])
        copy.start()
        mix_copies.append(copy)
        rs_y(index).start()
        turn(n2.at[index], n2_t, index)
        turn(dy, dy_t, index)
        if index + 1 < z_size:
            dy_loads[index + 1].start()

    def rs_y(index):
        return remote(
            gn_part.at[index, 1 - me_y], gn_y.at[index], rs_y_send.at[index], rs_y_recv.at[index], to_y
        )

    def rs_z(index):
        return remote(
            gn_s.at[index - 1],
            gn_z.at[index - 1],
            rs_z_send.at[index],
            rs_z_recv.at[index - 1],
            to_z(1),
        )

    def rs_step(index):
        rs_y(index).wait_recv()
        slot = (index - 2) % z_size
        if index != 1:
            remote(
                gn_s.at[slot], gn_z.at[slot], rs_z_send.at[1], rs_z_recv.at[slot], to_z(1)
            ).wait_recv()

        def add_tile(tile, carry):
            at = pl.ds(pl.multiple_of(tile * TILE, TILE), TILE)
            total = gn_part[index, me_y, at, :].astype(jnp.float32) + gn_y[index, at, :].astype(
                jnp.float32
            )
            if index != 1:
                total = total + gn_z[slot, at, :].astype(jnp.float32)
            if index == 0:
                gn_ref[:, at] = total.T
            else:
                gn_s[index - 1, at, :] = total.astype(jnp.bfloat16)
            return carry

        lax.fori_loop(0, width // TILE, add_tile, 0)
        if index != 0:
            rs_z(index).start()


    def grads(step):
        at = pl.ds(pl.multiple_of(ahead(step) * span, 128), span)
        for kind, source in enumerate((n2_t, n2_t, dy_t)):

            def tile_body(tile, carry, kind=kind, source=source):
                cols = pl.ds(pl.multiple_of(tile * WIDE, WIDE), WIDE)
                w3[kind, at, cols] = dot_nn(source[at, :], h3[kind, :, cols]).astype(jnp.bfloat16)
                return carry

            lax.fori_loop(0, units // WIDE, tile_body, 0)
        for far in (1, 0):
            for kind in range(3):
                over_c(kind, step, far).start()

    def over_c(kind, step, far):
        x_at = 1 - me_x if far else me_x
        return remote(
            w3.at[kind, row_block(ahead(step), x_at, 1 - me_c)],
            c_in.at[kind, step, far],
            c_send.at[kind, step, far],
            c_recv.at[kind, step, far],
            to_c,
        )

    def over_x(kind):
        return remote(
            w3.at[kind, row_block(ahead(1), 1 - me_x, me_c)],
            x_in.at[kind],
            x_send.at[kind],
            x_recv.at[kind],
            to_x,
        )

    out_copies = []

    def keep(kind, step, far, block):
        copy = pltpu.make_async_copy(
            block, sums_hbm.at[kind, step, far], out_sem.at[kind, step, far]
        )
        copy.start()
        out_copies.append(copy)

    def core_sums(step):
        for far in (1, 0):
            for kind in range(3):
                over_c(kind, step, far).wait_recv()
                x_at = 1 - me_x if far else me_x
                block = w3.at[kind, row_block(ahead(step), x_at, me_c)]
                add_rows(block, [c_in.at[kind, step, far]], block, rows)
                if step != 1:
                    keep(kind, step, far, block)
                elif far:
                    over_x(kind).start()

    def first_sums():
        for kind in range(3):
            over_x(kind).wait_recv()
            block = w3.at[kind, row_block(ahead(1), me_x, me_c)]
            add_rows(block, [x_in.at[kind]], block, rows)
            keep(kind, 1, 0, block)

    forward(1)
    for load in loads:
        load.wait()
    chunk(0)
    forward(2)
    chunk(1)
    forward(3)
    chunk(2)
    rs_step(1)
    chunk(3)
    rs_step(2)
    grads(1)
    grads(2)
    core_sums(1)
    rs_step(3)
    grads(3)
    core_sums(2)
    grads(0)
    core_sums(3)
    rs_step(0)
    core_sums(0)
    first_sums()

    for copy in mix_copies[3:] + out_copies:
        copy.wait()
    for index in range(z_size):
        if index:
            ag_y(index).wait_send()
        rs_y(index).wait_send()
        if index < z_size - 1:
            ag_z(index).wait_send()
        if index:
            rs_z(index).wait_send()
        for kind in range(3):
            over_c(kind, index, 0).wait_send()
            over_c(kind, index, 1).wait_send()
            if index == 1:
                over_x(kind).wait_send()


def ffn_call(normed, grad_all, weights, rows, main):
    z_size = lax.axis_size("z")
    pair, width = normed.shape
    units = weights.shape[2]
    own = pair // 2
    wide = lambda *lead: pltpu.VMEM((*lead, width), jnp.bfloat16)
    tall = lambda *lead: pltpu.VMEM((*lead, width, own), jnp.bfloat16)
    dma = lambda *lead: pltpu.SemaphoreType.DMA(lead)
    vmem = pl.BlockSpec(memory_space=pltpu.VMEM)
    hbm = pl.BlockSpec(memory_space=pl.ANY)
    return pl.pallas_call(
        functools.partial(ffn_kernel, z_size, main),
        out_shape=(
            jax.ShapeDtypeStruct((own, width), jnp.float32),
            jax.ShapeDtypeStruct((z_size, 2, width, own), jnp.bfloat16),
            jax.ShapeDtypeStruct((3, z_size, 2, rows, units), jnp.bfloat16),
        ),
        in_specs=[hbm, hbm, hbm],
        out_specs=(vmem, hbm, hbm),
        scratch_shapes=[
            wide(z_size, pair),
            wide(pair),
            pltpu.VMEM(weights.shape, jnp.bfloat16),
            pltpu.VMEM((3, z_size * pair, units), jnp.bfloat16),
            pltpu.VMEM((width, z_size * pair), jnp.bfloat16),
            pltpu.VMEM((width, z_size * pair), jnp.bfloat16),
            tall(z_size, 2),
            tall(2),
            tall(z_size),
            tall(z_size - 1),
            tall(z_size - 1),
            pltpu.VMEM((3, z_size, 2, rows, units), jnp.bfloat16),
            pltpu.VMEM((3, rows, units), jnp.bfloat16),
            dma(z_size + 4),
            dma(z_size),
            dma(z_size),
            dma(z_size),
            dma(z_size),
            dma(z_size),
            dma(z_size),
            dma(z_size),
            dma(z_size),
            dma(z_size),
            dma(3, z_size, 2),
            dma(3, z_size, 2),
            dma(3),
            dma(3),
            dma(3, z_size, 2),
        ],
        compiler_params=pltpu.CompilerParams(
            collective_id=0, has_side_effects=True, vmem_limit_bytes=VMEM_BYTES
        ),
        cost_estimate=pl.CostEstimate(
            flops=18 * z_size * pair * width * units,
            bytes_accessed=4 * weights.size + 12 * z_size * pair * width,
            transcendentals=z_size * pair * units,
        ),
    )(normed, grad_all, weights)


def spin(values, table):
    first = values[:, : values.shape[1] // 2]
    turned = first * table[0] + pltpu.roll(first, first.shape[1] // 2, 1) * table[1]
    return jnp.concatenate([turned, values[:, values.shape[1] // 2 :]], axis=1)


def spin_back(values, table):
    first = values[:, : values.shape[1] // 2]
    turned = first * table[0] - pltpu.roll(first, first.shape[1] // 2, 1) * table[1]
    return jnp.concatenate([turned, values[:, values.shape[1] // 2 :]], axis=1)


def head_probs(rotated, keys, allowed):
    scores = jnp.where(allowed > 0.5, matmul_nt(rotated, keys), masked_score)
    weights = jnp.exp(scores - jnp.max(scores, axis=-1, keepdims=True))
    return weights / jnp.sum(weights, axis=-1, keepdims=True)


def ragged_split(columns, parts):
    main = columns // parts // 128 * 128
    return main, main + 128


def pre_kernel(
    z_size,
    tok_ref,
    wkv_ref,
    gains_ref,
    table_ref,
    seg_ref,
    cot_hbm,
    wq_hbm,
    wo_hbm,
    wg_hbm,
    wu_hbm,
    wd_hbm,
    n1_ref,
    rot_ref,
    key_ref,
    val_ref,
    att_ref,
    mid_ref,
    n2_ref,
    gain_ref,
    allow_ref,
    kv_out,
    wq_out,
    wo_out,
    w3_out,
    dy_out,
    kv_w,
    q_w,
    o_w,
    tok,
    part,
    part_y,
    query,
    y_send,
    y_recv,
    az_send,
    az_recv,
    ax_send,
    ax_recv,
    ac_send,
    ac_recv,
    fz_send,
    fz_recv,
    fx_send,
    fx_recv,
    fc_send,
    fc_recv,
    dz_send,
    dz_recv,
    dy_send,
    dy_recv,
    local_sem,
):
    me_z, me_x = lax.axis_index("z"), lax.axis_index("x")
    me_c, me_y = lax.axis_index("c"), lax.axis_index("mp")
    own, width = tok_ref.shape
    rows = wq_hbm.shape[0]
    half_rows = wkv_ref.shape[0]
    head = key_ref.shape[1]
    main, units = ragged_split(wg_hbm.shape[1], z_size)
    to_y, to_x, to_c = {"mp": 1 - me_y}, {"x": 1 - me_x}, {"c": 1 - me_c}

    def to_z(step):
        return {"z": lax.rem(me_z + step, z_size)}

    def from_z(step):
        return lax.rem(me_z - step + z_size, z_size)

    def row_block(step, x_at, c_at):
        start = ((from_z(step) * 2 + x_at) * 2 + c_at) * rows
        return pl.ds(pl.multiple_of(start, rows), rows)

    mine = pl.ds(pl.multiple_of(me_y * own, own), own)
    theirs = pl.ds(pl.multiple_of((1 - me_y) * own, own), own)
    bufs = (kv_w, q_w, o_w)
    inputs = (None, wq_hbm, wo_hbm)

    locals_ = []

    def local(src, dst):
        copy = pltpu.make_async_copy(src, dst, local_sem.at[len(locals_)])
        copy.start()
        locals_.append(copy)
        return copy

    here = row_block(0, me_x, me_c)
    own_q = local(wq_hbm, q_w.at[here])
    own_o = local(wo_hbm, o_w.at[here])
    ffn_in = (wg_hbm, wu_hbm, wd_hbm)

    def pieces(target):
        yield pl.ds(pl.multiple_of(target * main, 128), main), pl.ds(0, main)
        tail = (z_size * main) + (target // 2) * 128
        yield pl.ds(pl.multiple_of(tail, 128), 128), pl.ds(main, 128)

    own_f = []
    for kind in range(3):
        for src, dst in pieces(me_z):
            own_f.append(local(ffn_in[kind].at[:, src], w3_out.at[kind, here, dst]))
    own_d = local(cot_hbm, dy_out.at[0, mine])

    barrier = pltpu.get_barrier_semaphore()
    peers = [to_y, to_x, to_c] + [to_z(step) for step in range(1, z_size)]
    for where in peers:
        pl.semaphore_signal(barrier, inc=1, device_id=where, device_id_type=MESH_ID)
    pl.semaphore_wait(barrier, len(peers))

    kv_mine = pl.ds(pl.multiple_of(here.start + me_y * half_rows, half_rows), half_rows)
    kv_theirs = pl.ds(pl.multiple_of(here.start + (1 - me_y) * half_rows, half_rows), half_rows)
    kv_block, kv_other = kv_w.at[kv_mine], kv_w.at[kv_theirs]
    kv_y = remote(kv_block, kv_block, y_send.at[0], y_recv.at[0], to_y)
    kv_y_in = remote(kv_other, kv_other, y_send.at[0], y_recv.at[0], to_y)
    tok_y = remote(tok_ref, tok.at[mine], y_send.at[1], y_recv.at[1], to_y)
    tok_y_in = remote(tok_ref, tok.at[theirs], y_send.at[1], y_recv.at[1], to_y)
    part_out = remote(part.at[theirs], part_y, y_send.at[2], y_recv.at[2], to_y)
    n2_y = remote(n2_ref.at[mine], n2_ref.at[mine], y_send.at[3], y_recv.at[3], to_y)
    n2_y_in = remote(n2_ref.at[theirs], n2_ref.at[theirs], y_send.at[3], y_recv.at[3], to_y)

    def source(kind, step):
        if isinstance(step, int) and step == 0 and kind:
            return inputs[kind]
        return bufs[kind].at[row_block(step, me_x, me_c)]

    first_z, last_z = (z_size - 1 - me_z) // (z_size - 1), me_z // (z_size - 1)
    inner = first_z + last_z == 0
    order = (0, 1 + 2 * first_z, 3 - first_z - last_z, 2 - first_z + last_z)
    hops = (
        None,
        (lax.rem(me_z + 1, z_size), 2),
        (lax.rem(me_z + z_size - 1, z_size), 2),
        (lax.rem(3 * (me_z + 3), z_size), lax.rem(2 * me_z + 3, z_size)),
    )

    def a_z_own(kind, right):
        return remote(
            source(kind, 0),
            bufs[kind].at[here],
            az_send.at[kind, right],
            az_recv.at[kind, 1 if right else z_size - 1],
            to_z(1 if right else z_size - 1),
        )

    def a_z_start(kind):
        @pl.when(last_z == 0)
        def _():
            a_z_own(kind, 1).start()

        @pl.when(first_z == 0)
        def _():
            a_z_own(kind, 0).start()

    def a_z(kind, index):
        target, slot = hops[index]
        block = bufs[kind].at[row_block(order[index], me_x, me_c)]
        return remote(
            block, block, az_send.at[kind, 1 + index], az_recv.at[kind, slot], {"z": target}
        )

    def a_z_next(kind, index):
        @pl.when(inner)
        def _():
            a_z(kind, index).start()

    def a_z_done(kind):
        @pl.when(last_z == 0)
        def _():
            a_z_own(kind, 1).wait_send()

        @pl.when(first_z == 0)
        def _():
            a_z_own(kind, 0).wait_send()

        @pl.when(inner)
        def _():
            for index in range(1, z_size):
                a_z(kind, index).wait_send()

    def a_z_in(kind, step):
        block = bufs[kind].at[row_block(step, me_x, me_c)]
        return remote(block, block, az_send.at[kind, 0], az_recv.at[kind, step], to_z(1))

    def a_x(kind, step):
        return remote(
            source(kind, step),
            bufs[kind].at[row_block(step, me_x, me_c)],
            ax_send.at[kind, step],
            ax_recv.at[kind, step],
            to_x,
        )

    def a_x_in(kind, step):
        block = bufs[kind].at[row_block(step, 1 - me_x, me_c)]
        return remote(block, block, ax_send.at[kind, step], ax_recv.at[kind, step], to_x)

    def a_c(kind, step, far):
        x_at = 1 - me_x if far else me_x
        block = bufs[kind].at[row_block(step, x_at, me_c)]
        src = block if far else source(kind, step)
        slot = step + z_size * far
        return remote(src, block, ac_send.at[kind, slot], ac_recv.at[kind, slot], to_c)

    def a_c_in(kind, step, far):
        x_at = 1 - me_x if far else me_x
        block = bufs[kind].at[row_block(step, x_at, 1 - me_c)]
        slot = step + z_size * far
        return remote(block, block, ac_send.at[kind, slot], ac_recv.at[kind, slot], to_c)

    def f_z(kind, step):
        target = lax.rem(me_z + step, z_size)
        return [
            remote(
                ffn_in[kind].at[:, src],
                w3_out.at[kind, here, dst],
                fz_send.at[kind, step, index],
                fz_recv.at[kind, step, index],
                to_z(step),
            )
            for index, (src, dst) in enumerate(pieces(target))
        ]

    def f_z_in(kind, step):
        block = row_block(step, me_x, me_c)
        return [
            remote(
                w3_out.at[kind, block, dst],
                w3_out.at[kind, block, dst],
                fz_send.at[kind, step, index],
                fz_recv.at[kind, step, index],
                to_z(step),
            )
            for index, (_, dst) in enumerate(pieces(me_z))
        ]

    def f_x(kind, step):
        block = w3_out.at[kind, row_block(step, me_x, me_c)]
        return remote(block, block, fx_send.at[kind, step], fx_recv.at[kind, step], to_x)

    def f_x_in(kind, step):
        block = w3_out.at[kind, row_block(step, 1 - me_x, me_c)]
        return remote(block, block, fx_send.at[kind, step], fx_recv.at[kind, step], to_x)

    def f_c(kind, step, far):
        block = w3_out.at[kind, row_block(step, 1 - me_x if far else me_x, me_c)]
        slot = step + z_size * far
        return remote(block, block, fc_send.at[kind, slot], fc_recv.at[kind, slot], to_c)

    def f_c_in(kind, step, far):
        block = w3_out.at[kind, row_block(step, 1 - me_x if far else me_x, 1 - me_c)]
        slot = step + z_size * far
        return remote(block, block, fc_send.at[kind, slot], fc_recv.at[kind, slot], to_c)

    def d_source(step):
        return cot_hbm if isinstance(step, int) else dy_out.at[step, mine]

    def d_z_own(right):
        slot = 1 if right else z_size - 1
        return remote(
            cot_hbm, dy_out.at[slot, mine], dz_send.at[right], dz_recv.at[slot], to_z(slot)
        )

    def d_z_start():
        @pl.when(last_z == 0)
        def _():
            d_z_own(1).start()

        @pl.when(first_z == 0)
        def _():
            d_z_own(0).start()

    def d_z(index):
        target, slot = hops[index]
        return remote(
            dy_out.at[order[index], mine],
            dy_out.at[slot, mine],
            dz_send.at[1 + index],
            dz_recv.at[slot],
            {"z": target},
        )

    def d_z_done():
        @pl.when(last_z == 0)
        def _():
            d_z_own(1).wait_send()

        @pl.when(first_z == 0)
        def _():
            d_z_own(0).wait_send()

        @pl.when(inner)
        def _():
            for index in range(1, z_size):
                d_z(index).wait_send()

    def d_z_in(step):
        block = dy_out.at[step, mine]
        return remote(block, block, dz_send.at[0], dz_recv.at[step], to_z(1))

    def d_y(step):
        return remote(
            d_source(step), dy_out.at[step, mine], dy_send.at[step], dy_recv.at[step], to_y
        )

    def d_y_in(step):
        block = dy_out.at[step, theirs]
        return remote(block, block, dy_send.at[step], dy_recv.at[step], to_y)

    spread = jnp.concatenate([gains_ref[...], jnp.zeros((120, 128), jnp.float32)], axis=0).T
    kv_w[kv_mine, : 2 * head] = wkv_ref[...]
    kv_w[kv_mine, 2 * head :] = spread[:half_rows, :].astype(jnp.bfloat16)
    kv_y.start()
    tok_y.start()
    for kind in (1, 2):
        a_z_start(kind)
        a_x(kind, 0).start()
        a_c(kind, 0, 0).start()
    tok[mine, :] = tok_ref[...]
    seq = 2 * own
    query_at = lax.broadcasted_iota(jnp.int32, (seq, seq), 0)
    key_at = lax.broadcasted_iota(jnp.int32, (seq, seq), 1)
    same = seg_ref[...].T[:, :1] == seg_ref[:1, :]
    allowed = same & (key_at <= query_at) & (query_at - key_at < WINDOW)
    allow_ref[...] = jnp.where(allowed, 1.0, 0.0)
    kv_y_in.wait_recv()
    a_z_start(0)
    a_x(0, 0).start()
    a_c(0, 0, 0).start()
    d_y(0).start()
    for step in range(1, z_size):
        for kind in (1, 0, 2):
            a_z_in(kind, order[step]).wait_recv()
            a_z_next(kind, step)
            a_x(kind, order[step]).start()
            a_c(kind, order[step], 0).start()
        if step == z_size - 2:
            d_z_start()
        if step == z_size - 1:
            for copy in own_f:
                copy.wait()
            for kind in range(3):
                for away in (1, 3, 2):
                    for copy in f_z(kind, away):
                        copy.start()
            for kind in range(3):
                f_x(kind, 0).start()
                f_c(kind, 0, 0).start()
        for kind in (1, 0, 2):
            a_x_in(kind, order[step - 1]).wait_recv()
            a_c(kind, order[step - 1], 1).start()

    def hand_on(kind, step):
        for copy in f_z_in(kind, step):
            copy.wait_recv()
        f_x(kind, step).start()
        f_c(kind, step, 0).start()

    def cross(kind, step):
        f_x_in(kind, step).wait_recv()
        f_c(kind, step, 1).start()

    def pass_cotangent(step):
        d_z_in(order[step]).wait_recv()

        @pl.when(inner)
        def _():
            d_z(step).start()

        d_y(order[step]).start()

    for kind in (1, 0, 2):
        a_x_in(kind, order[z_size - 1]).wait_recv()
        a_c(kind, order[z_size - 1], 1).start()
    tok_y_in.wait_recv()
    own_q.wait()
    own_o.wait()
    for kind in (0, 1):
        for step in range(z_size):
            for far in range(2):
                a_c_in(kind, step, far).wait_recv()

    gains = kv_w[:, 2 * head :].astype(jnp.float32).T[:8, :]
    gain_ref[...] = gains

    def norm_rows(index, carry):
        at = pl.ds(pl.multiple_of(index * 32, 32), 32)
        values = tok[at, :].astype(jnp.float32)
        scale = lax.rsqrt(jnp.mean(values * values, axis=-1, keepdims=True) + epsilon)
        n1_ref[at, :] = (values * scale * gain_ref[0:1, :]).astype(jnp.bfloat16)
        return carry

    lax.fori_loop(0, 2 * own // 32, norm_rows, 0)
    hand_on(0, 1)
    table = (table_ref[0], table_ref[1])
    key_ref[...] = spin(dot_nn(n1_ref[...], kv_w[:, :head]), table).astype(jnp.bfloat16)
    val_ref[...] = dot_nn(n1_ref[...], kv_w[:, head : 2 * head]).astype(jnp.bfloat16)
    hand_on(0, 3)
    head_scale = head ** (-0.5)
    heads = att_ref.shape[1] // head

    half_cols = att_ref.shape[1] // 2
    for index in range(2):
        cols = pl.ds(index * half_cols, half_cols)
        query[:, cols] = dot_nn(n1_ref[...], q_w[:, cols])

    def attend(index):
        cols = pl.ds(index * head, head)
        rotated = (spin(query[:, cols], table) * head_scale).astype(jnp.bfloat16)
        rot_ref[:, cols] = rotated
        probs = head_probs(rotated, key_ref[...], allow_ref[...]).astype(jnp.bfloat16)
        att_ref[:, cols] = dot_nn(probs, val_ref[...]).astype(jnp.bfloat16)

    tasks = [
        lambda: hand_on(0, 2),
        lambda: pass_cotangent(1),
        lambda: hand_on(1, 1),
        lambda: cross(0, 0),
        lambda: hand_on(1, 3),
    ]
    for index in range(heads):
        attend(index)
        if index < len(tasks):
            tasks[index]()
    for step in range(z_size):
        for far in range(2):
            a_c_in(2, step, far).wait_recv()
    saves = [
        local(kv_w, kv_out),
        local(q_w, wq_out),
        local(o_w, wo_out),
    ]
    span = width // 4

    def project(index, carry):
        cols = pl.ds(pl.multiple_of(index * span, span), span)
        part[:, cols] = matmul_nt(att_ref[...], o_w[cols, :]).astype(jnp.bfloat16)
        return carry

    lax.fori_loop(0, 4, project, 0)
    part_out.start()
    hand_on(1, 2)
    cross(1, 0)
    cross(2, 0)
    cross(0, 1)
    pass_cotangent(2)
    hand_on(2, 1)
    part_out.wait_recv()

    def middle(index, carry):
        at = pl.ds(pl.multiple_of(index * 32, 32), 32)
        there = pl.ds(pl.multiple_of(me_y * own + index * 32, 32), 32)
        values = (
            tok_ref[at, :].astype(jnp.float32)
            + part[there, :].astype(jnp.float32)
            + part_y[at, :].astype(jnp.float32)
        )
        mid_ref[at, :] = values
        scale = lax.rsqrt(jnp.mean(values * values, axis=-1, keepdims=True) + epsilon)
        n2_ref[there, :] = (values * scale * gain_ref[1:2, :]).astype(jnp.bfloat16)
        return carry

    lax.fori_loop(0, own // 32, middle, 0)
    n2_y.start()
    hand_on(2, 3)
    cross(0, 3)
    pass_cotangent(3)
    hand_on(2, 2)
    cross(0, 2)
    for kind in (1, 2):
        for step in (1, 3, 2):
            cross(kind, step)
    for kind in range(3):
        for step in range(z_size):
            for far in range(2):
                f_c_in(kind, step, far).wait_recv()
    for step in range(z_size):
        d_y_in(step).wait_recv()
    n2_y_in.wait_recv()

    for kind in range(3):
        a_z_done(kind)
    d_z_done()
    kv_y.wait_send()
    tok_y.wait_send()
    part_out.wait_send()
    n2_y.wait_send()
    own_d.wait()
    for copy in saves:
        copy.wait()
    for step in range(z_size):
        d_y(step).wait_send()
        for kind in range(3):
            if step:
                for copy in f_z(kind, step):
                    copy.wait_send()
            a_x(kind, step).wait_send()
            f_x(kind, step).wait_send()
            for far in range(2):
                a_c(kind, step, far).wait_send()
                f_c(kind, step, far).wait_send()


def pre_call(tokens, w_kv, gains, table, segments, cotangent, w_query, w_out, ffn):
    z_size = lax.axis_size("z")
    own, width = tokens.shape
    seq = 2 * own
    rows, cols = w_query.shape
    head = table.shape[2] * 2
    units = ragged_split(ffn[0].shape[1], z_size)[1]
    low = lambda *dims: jax.ShapeDtypeStruct(dims, jnp.bfloat16)
    full = lambda *dims: jax.ShapeDtypeStruct(dims, jnp.float32)
    dma = lambda *lead: pltpu.SemaphoreType.DMA(lead)
    vmem = pl.BlockSpec(memory_space=pltpu.VMEM)
    hbm = pl.BlockSpec(memory_space=pl.ANY)
    wide = lambda *lead: pltpu.VMEM((*lead, width), jnp.bfloat16)
    return pl.pallas_call(
        functools.partial(pre_kernel, z_size),
        out_shape=(
            low(seq, width),
            low(seq, cols),
            low(seq, head),
            low(seq, head),
            low(seq, cols),
            full(own, width),
            low(seq, width),
            full(8, width),
            full(seq, seq),
            low(width, 2 * head + 128),
            low(width, cols),
            low(width, cols),
            low(3, width, units),
            low(z_size, seq, width),
        ),
        in_specs=[vmem] * 5 + [hbm] * 6,
        out_specs=(vmem,) * 9 + (hbm,) * 5,
        scratch_shapes=[
            pltpu.VMEM((width, 2 * head + 128), jnp.bfloat16),
            pltpu.VMEM((width, cols), jnp.bfloat16),
            pltpu.VMEM((width, cols), jnp.bfloat16),
            wide(seq),
            wide(seq),
            wide(own),
            pltpu.VMEM((seq, cols), jnp.float32),
            dma(4),
            dma(4),
            dma(3, z_size + 1),
            dma(3, z_size),
            dma(3, z_size),
            dma(3, z_size),
            dma(3, 2 * z_size),
            dma(3, 2 * z_size),
            dma(3, z_size, 2),
            dma(3, z_size, 2),
            dma(3, z_size),
            dma(3, z_size),
            dma(3, 2 * z_size),
            dma(3, 2 * z_size),
            dma(z_size + 1),
            dma(z_size),
            dma(z_size),
            dma(z_size),
            dma(16),
        ],
        compiler_params=pltpu.CompilerParams(
            collective_id=1, has_side_effects=True, vmem_limit_bytes=VMEM_BYTES
        ),
        cost_estimate=pl.CostEstimate(
            flops=8 * seq * width * cols,
            bytes_accessed=8 * width * (cols + units),
            transcendentals=seq * seq * cols // head,
        ),
    )(tokens, w_kv, gains, table, segments, cotangent, w_query, w_out, *ffn)


def norm_back(values, gain, upstream):
    scale = lax.rsqrt(jnp.mean(values * values, axis=-1, keepdims=True) + epsilon)
    normed = values * scale
    pulled = gain * upstream
    back = scale * (pulled - normed * jnp.mean(normed * pulled, axis=-1, keepdims=True))
    return back, jnp.sum(upstream * normed, axis=0, keepdims=True)


def post_kernel(
    z_size,
    mid_ref,
    tok_ref,
    cot_ref,
    gain_ref,
    n1_ref,
    rot_ref,
    key_ref,
    val_ref,
    att_ref,
    table_ref,
    allow_ref,
    kv_hbm,
    wq_hbm,
    wo_hbm,
    mix_hbm,
    gn_hbm,
    sums_hbm,
    mixed_ref,
    tgrad_ref,
    gsum_ref,
    kvg_ref,
    qg_ref,
    og_ref,
    ffn_out,
    kv_w,
    q_w,
    o_w,
    o_part,
    gm,
    gm_f,
    gq,
    gkv,
    kv_sum,
    back_y,
    mix_y,
    mix_z,
    mix_s,
    o_c,
    o_x,
    o_z,
    q_c,
    q_x,
    q_z,
    kv_y,
    kv_c,
    kv_x,
    kv_z,
    gain_own,
    gain_in,
    ffn_in,
    ffn_own,
    load_sem,
    own_sem,
    fx_send,
    fx_recv,
    fz_send,
    fz_recv,
    y_send,
    y_recv,
    my_send,
    my_recv,
    mz_send,
    mz_recv,
    wc_send,
    wc_recv,
    wx_send,
    wx_recv,
    wz_send,
    wz_recv,
    kc_send,
    kc_recv,
    kz_send,
    kz_recv,
    g_send,
    g_recv,
):
    me_z, me_x = lax.axis_index("z"), lax.axis_index("x")
    me_c, me_y = lax.axis_index("c"), lax.axis_index("mp")
    own, width = tok_ref.shape
    seq = 2 * own
    head = key_ref.shape[1]
    cols_here = att_ref.shape[1]
    heads = cols_here // head
    rows = qg_ref.shape[0]
    span = width // z_size
    mine = pl.ds(pl.multiple_of(me_y * own, own), own)
    theirs = pl.ds(pl.multiple_of((1 - me_y) * own, own), own)
    to_y, to_x, to_c = {"mp": 1 - me_y}, {"x": 1 - me_x}, {"c": 1 - me_c}
    head_scale = head ** (-0.5)

    def behind(step):
        return lax.rem(me_z - step + z_size, z_size)

    def to_z(step):
        return {"z": lax.rem(me_z + step, z_size)}

    def row_block(step, x_at, c_at):
        start = ((behind(step) * 2 + x_at) * 2 + c_at) * rows
        return pl.ds(pl.multiple_of(start, rows), rows)

    loads = [
        pltpu.make_async_copy(wo_hbm, o_w, load_sem.at[0]),
        pltpu.make_async_copy(wq_hbm, q_w, load_sem.at[1]),
        pltpu.make_async_copy(
            kv_hbm.at[:, :, :, :, :, pl.ds(0, 2 * head)], kv_w, load_sem.at[2]
        ),
    ]
    for step in range(z_size):
        loads.append(
            pltpu.make_async_copy(mix_hbm.at[step, me_y], mix_s.at[step], load_sem.at[3 + step])
        )
    gn_load = pltpu.make_async_copy(gn_hbm, gm_f, load_sem.at[3 + z_size])
    gn_load.start()
    for load in loads:
        load.start()

    barrier = pltpu.get_barrier_semaphore()
    peers = [to_y, to_x, to_c] + [to_z(step) for step in range(1, z_size)]
    for where in peers:
        pl.semaphore_signal(barrier, inc=1, device_id=where, device_id_type=MESH_ID)
    pl.semaphore_wait(barrier, len(peers))

    tasks = [(step, kind) for step in (2, 3) for kind in range(3)]

    def f_x(index):
        step, kind = tasks[index]
        return remote(
            sums_hbm.at[kind, step, 1],
            ffn_in.at[index],
            fx_send.at[index],
            fx_recv.at[index],
            to_x,
        )

    def f_own(index):
        step, kind = tasks[index]
        return pltpu.make_async_copy(
            sums_hbm.at[kind, step, 0], ffn_own.at[index % 2], own_sem.at[index % 2]
        )

    def f_z(step, kind):
        if step == 1:
            src = sums_hbm.at[kind, 1, 0]
        else:
            src = ffn_in.at[tasks.index((step, kind))]
        return remote(
            src, ffn_out.at[kind, step], fz_send.at[kind, step], fz_recv.at[kind, step], to_z(step)
        )

    def tick(index):
        step, kind = tasks[index]
        f_x(index).wait_recv()
        f_own(index).wait()
        block = ffn_in.at[index]
        add_rows(block, [ffn_own.at[index % 2]], block, rows)
        if index + 2 < len(tasks):
            f_own(index + 2).start()
        f_z(step, kind).start()

    def f_x_own(kind):
        return remote(
            sums_hbm.at[kind, 0, 1],
            ffn_out.at[kind, 0],
            fx_send.at[len(tasks) + kind],
            fx_recv.at[len(tasks) + kind],
            to_x,
        )

    f_own(0).start()
    f_own(1).start()
    for index in range(len(tasks)):
        f_x(index).start()
    for kind in range(3):
        f_z(1, kind).start()

    gn_load.wait()

    def mid_rows(index, total):
        at = pl.ds(pl.multiple_of(index * 32, 32), 32)
        grad, gain_part = norm_back(mid_ref[at, :], gain_ref[1:2, :], gm_f[at, :])
        grad = grad + cot_ref[at, :].astype(jnp.float32)
        gm_f[at, :] = grad
        gm[pl.ds(pl.multiple_of(me_y * own + index * 32, 32), 32), :] = grad.astype(jnp.bfloat16)
        return total + gain_part

    ffn_gain_part = lax.fori_loop(
        0, own // 32, mid_rows, jnp.zeros((1, width), jnp.float32)
    )
    gm_y = remote(gm.at[mine], gm.at[mine], y_send.at[0], y_recv.at[0], to_y)
    gm_y_in = remote(gm.at[theirs], gm.at[theirs], y_send.at[0], y_recv.at[0], to_y)
    gm_y.start()

    def mix_over_y(step):
        return remote(
            mix_hbm.at[step, 1 - me_y], mix_y.at[step], my_send.at[step], my_recv.at[step], to_y
        )

    def mix_over_z(step):
        return remote(
            mix_s.at[step], mix_z.at[step - 1], mz_send.at[step], mz_recv.at[step - 1], to_z(1)
        )

    def mix_step(step):
        mix_over_y(step).wait_recv()
        slot = (step - 2) % z_size
        others = [mix_y.at[step]]
        if step != 1:
            remote(
                mix_s.at[1], mix_z.at[slot], mz_send.at[1], mz_recv.at[slot], to_z(1)
            ).wait_recv()
            others.append(mix_z.at[slot])
        if step:
            def add_tile(tile, carry):
                at = pl.ds(pl.multiple_of(tile * TILE, TILE), TILE)
                total = mix_s[step, at, :].astype(jnp.float32)
                for other in others:
                    total = total + other[at, :].astype(jnp.float32)
                mix_s[step, at, :] = total.astype(jnp.bfloat16)
                return carry

            lax.fori_loop(0, width // TILE, add_tile, 0)
            mix_over_z(step).start()
        else:
            def last_tile(tile, carry):
                at = pl.ds(pl.multiple_of(tile * TILE, TILE), TILE)
                total = mix_s[0, at, :].astype(jnp.float32)
                for other in others:
                    total = total + other[at, :].astype(jnp.float32)
                mixed_ref[:, at] = (mid_ref[:, at] + total.T).astype(jnp.bfloat16)
                return carry

            lax.fori_loop(0, width // TILE, last_tile, 0)

    for step in (1, 2, 3, 0):
        mix_over_y(step).start()

    kinds = ((o_part, o_c, o_x, o_z, og_ref), (o_w, q_c, q_x, q_z, qg_ref))

    def w_c(kind, step, far):
        x_at = 1 - me_x if far else me_x
        return remote(
            kinds[kind][0].at[row_block(step, x_at, 1 - me_c)],
            kinds[kind][1].at[step, far],
            wc_send.at[kind, step, far],
            wc_recv.at[kind, step, far],
            to_c,
        )

    def w_x(kind, step):
        return remote(
            kinds[kind][0].at[row_block(step, 1 - me_x, me_c)],
            kinds[kind][2].at[step],
            wx_send.at[kind, step],
            wx_recv.at[kind, step],
            to_x,
        )

    first_z, last_z = (z_size - 1 - me_z) // (z_size - 1), me_z // (z_size - 1)
    inner = first_z + last_z == 0
    order = (
        0,
        1 + (me_z + 1) // 2,
        2 + (2 * me_z - 3) * (1 - first_z - last_z),
        3 - 2 * (me_z // 2),
    )
    right = (None, 1 - me_z // 2, (3 - me_z) * (2 - me_z) // 6 + me_z // 2 * (1 - last_z), 1 - me_z // 2)

    def w_z(kind, index):
        step, way = order[index], right[index]
        slot = way * lax.rem(step + 1, z_size) + (1 - way) * (step - 1 + 4 * ((3 - step) // 2))
        return remote(
            kinds[kind][0].at[row_block(step, me_x, me_c)],
            kinds[kind][3].at[slot],
            wz_send.at[kind, index],
            wz_recv.at[kind, slot],
            {"z": me_z + 2 * way - 1},
        )

    def w_z_in(kind, slot):
        block = kinds[kind][3].at[slot]
        return remote(block, block, wz_send.at[kind, 1], wz_recv.at[kind, slot], to_z(1))

    def w_x_stage(kind, index):
        step = order[index]
        w_c(kind, step, 1).wait_recv()
        block = kinds[kind][0].at[row_block(step, 1 - me_x, me_c)]
        add_rows(block, [kinds[kind][1].at[step, 1]], block, rows)
        w_x(kind, step).start()

    def w_z_stage(kind, index):
        part, from_c, from_x, from_z, result = kinds[kind]
        step = order[index]
        w_c(kind, step, 0).wait_recv()
        w_x(kind, step).wait_recv()
        block = part.at[row_block(step, me_x, me_c)]
        others = [from_c.at[step, 0], from_x.at[step]]
        if index:

            @pl.when(inner)
            def _():
                w_z_in(kind, step).wait_recv()
                add_rows(block, [*others, from_z.at[step]], block, rows)

            @pl.when(first_z + last_z > 0)
            def _():
                add_rows(block, others, block, rows)

            w_z(kind, index).start()
        else:

            @pl.when(first_z == 0)
            def _():
                w_z_in(kind, 0).wait_recv()

            @pl.when(last_z == 0)
            def _():
                w_z_in(kind, z_size).wait_recv()

            @pl.when(inner)
            def _():
                add_rows(block, [*others, from_z.at[0], from_z.at[z_size]], result, rows)

            @pl.when(first_z > 0)
            def _():
                add_rows(block, [*others, from_z.at[z_size]], result, rows)

            @pl.when(last_z > 0)
            def _():
                add_rows(block, [*others, from_z.at[0]], result, rows)

    def w_product(kind, index, left, values):
        step = order[index]
        at = pl.ds(pl.multiple_of(behind(step) * span, 128), span)
        turned = left[:, at].T

        def tile_body(tile, carry):
            cols = pl.ds(pl.multiple_of(tile * TILE, TILE), TILE)
            kinds[kind][0][at, cols] = dot_nn(turned, values[:, cols]).astype(jnp.bfloat16)
            return carry

        lax.fori_loop(0, cols_here // TILE, tile_body, 0)
        for far in (1, 0):
            w_c(kind, step, far).start()

    tick(0)
    tick(1)
    gm_y_in.wait_recv()
    w_product(0, 1, gm, att_ref)
    w_product(0, 2, gm, att_ref)
    w_x_stage(0, 1)
    w_product(0, 3, gm, att_ref)
    w_x_stage(0, 2)
    tick(2)
    w_product(0, 0, gm, att_ref)
    w_x_stage(0, 3)
    for load in loads:
        load.wait()

    kv_sum[...] = jnp.zeros(kv_sum.shape, jnp.float32)
    table = (table_ref[0], table_ref[1])

    for index in range(2):
        cols = pl.ds(index * (cols_here // 2), cols_here // 2)
        gq[:, cols] = dot_nn(gm[...], o_w[:, cols]).astype(jnp.bfloat16)

    def attend_back(index):
        cols = pl.ds(index * head, head)
        grad_vals = gq[:, cols]
        rotated = rot_ref[:, cols]
        probs = head_probs(rotated, key_ref[...], allow_ref[...])
        grad_probs = matmul_nt(grad_vals, val_ref[...])
        delta = jnp.sum(probs * grad_probs, axis=-1, keepdims=True)
        grad_scores = (probs * (grad_probs - delta)).astype(jnp.bfloat16)
        grad_rot = dot_nn(grad_scores, key_ref[...])
        gq[:, cols] = (spin_back(grad_rot, table) * head_scale).astype(jnp.bfloat16)
        kv_sum[0] += matmul_tn(grad_scores, rotated)
        kv_sum[1] += matmul_tn(probs.astype(jnp.bfloat16), grad_vals)

    for index in range(heads):
        attend_back(index)
        if index == 0:
            w_x_stage(0, 0)
        if 3 + index < len(tasks):
            tick(3 + index)
        if index == heads - 1:
            mix_step(1)
    gkv[:, :head] = spin_back(kv_sum[0], table).astype(jnp.bfloat16)
    gkv[:, head:] = kv_sum[1].astype(jnp.bfloat16)

    w_product(1, 1, n1_ref, gq)
    w_product(1, 2, n1_ref, gq)
    w_x_stage(1, 1)
    w_z_stage(0, 1)
    w_product(1, 3, n1_ref, gq)
    w_x_stage(1, 2)
    w_product(1, 0, n1_ref, gq)
    w_x_stage(1, 3)
    w_x_stage(1, 0)
    for kind in range(3):
        f_x_own(kind).start()

    gm_y.wait_send()
    back = gm
    def input_tile(index, carry):
        at = pl.ds(pl.multiple_of(index * span, 128), span)
        back[:, at] = (
            matmul_nt(gq[...], q_w[at, :]) + matmul_nt(gkv[...], kv_w[index].reshape(span, 2 * head))
        ).astype(jnp.bfloat16)
        return carry

    lax.fori_loop(0, z_size, input_tile, 0)
    back_out = remote(back.at[theirs], back_y, y_send.at[1], y_recv.at[1], to_y)
    back_out.start()

    kv_part = kv_w

    def kv_tile(index, carry):
        at = pl.ds(pl.multiple_of(index * span, 128), span)
        product = dot_nn(n1_ref[:, at].T, gkv[...]).astype(jnp.bfloat16)
        kv_part[index] = product.reshape(kv_part.shape[1:])
        return carry

    lax.fori_loop(0, z_size, kv_tile, 0)
    kv_over_y = remote(kv_part.at[:, :, :, 1 - me_y], kv_y, y_send.at[2], y_recv.at[2], to_y)
    kv_over_y.start()
    mix_step(2)
    w_z_stage(0, 2)
    mix_step(3)
    w_z_stage(0, 3)

    back_out.wait_recv()

    def input_rows(index, total):
        at = pl.ds(pl.multiple_of(index * 32, 32), 32)
        there = pl.ds(pl.multiple_of(me_y * own + index * 32, 32), 32)
        upstream = back[there, :].astype(jnp.float32) + back_y[at, :].astype(jnp.float32)
        grad, gain_part = norm_back(
            tok_ref[at, :].astype(jnp.float32), gain_ref[0:1, :], upstream
        )
        tgrad_ref[at, :] = (gm_f[at, :] + grad).astype(jnp.bfloat16)
        return total + gain_part

    attn_gain_part = lax.fori_loop(
        0, own // 32, input_rows, jnp.zeros((1, width), jnp.float32)
    )
    for index in range(4):
        at = slice(index * span, (index + 1) * span)
        gain_own[0, index : index + 1, :] = attn_gain_part[:, at]
        gain_own[0, 4 + index : 5 + index, :] = ffn_gain_part[:, at]

    def gain_send(stage, where):
        return remote(
            gain_own.at[stage], gain_in.at[stage], g_send.at[stage], g_recv.at[stage], where
        )

    gain_hops = [gain_send(0, to_y), gain_send(1, to_c), gain_send(2, to_x)]
    gain_last = [
        remote(
            gain_own.at[3], gain_in.at[2 + step], g_send.at[2 + step], g_recv.at[2 + step], to_z(step)
        )
        for step in range(1, z_size)
    ]

    def gain_fold(stage):
        gain_hops[stage].wait_recv()
        gain_own[stage + 1] = gain_own[stage] + gain_in[stage]

    gain_hops[0].start()
    w_z_stage(1, 1)
    w_z_stage(0, 0)
    w_z_stage(1, 2)
    gain_fold(0)
    gain_hops[1].start()
    mix_step(0)
    w_z_stage(1, 3)
    gain_fold(1)
    gain_hops[2].start()
    kv_over_y.wait_recv()

    def kv_add_y(index, carry):
        for x_at in range(2):
            for c_at in range(2):
                block = kv_part.at[index, x_at, c_at, me_y]
                block[...] = (
                    block[...].astype(jnp.float32) + kv_y[index, x_at, c_at].astype(jnp.float32)
                ).astype(jnp.bfloat16)
        return carry

    lax.fori_loop(0, z_size, kv_add_y, 0)
    kv_over_c = remote(
        kv_part.at[:, :, 1 - me_c, me_y], kv_c, kc_send.at[0], kc_recv.at[0], to_c
    )
    kv_over_c.start()
    gain_fold(2)
    for copy in gain_last:
        copy.start()
    kv_over_c.wait_recv()

    def kv_add_c(index, carry):
        for x_at in range(2):
            block = kv_part.at[index, x_at, me_c, me_y]
            block[...] = (
                block[...].astype(jnp.float32) + kv_c[index, x_at].astype(jnp.float32)
            ).astype(jnp.bfloat16)
        return carry

    lax.fori_loop(0, z_size, kv_add_c, 0)
    kv_over_x = remote(
        kv_part.at[:, 1 - me_x, me_c, me_y], kv_x, kc_send.at[1], kc_recv.at[1], to_x
    )
    kv_over_x.start()
    w_z_stage(1, 0)
    kv_over_x.wait_recv()

    def kv_add_x(index, carry):
        block = kv_part.at[index, me_x, me_c, me_y]
        block[...] = (
            block[...].astype(jnp.float32) + kv_x[index].astype(jnp.float32)
        ).astype(jnp.bfloat16)
        return carry

    lax.fori_loop(0, z_size, kv_add_x, 0)
    kv_over_z = [
        remote(
            kv_part.at[lax.rem(me_z + step, z_size), me_x, me_c, me_y],
            kv_z.at[step - 1],
            kz_send.at[step],
            kz_recv.at[step],
            to_z(step),
        )
        for step in range(1, z_size)
    ]
    for copy in kv_over_z:
        copy.start()
    for copy in gain_last:
        copy.wait_recv()
    gsum_ref[...] = gain_own[3] + gain_in[3] + gain_in[4] + gain_in[5]
    for copy in kv_over_z:
        copy.wait_recv()
    kvg_ref[...] = (
        kv_part[me_z, me_x, me_c, me_y].astype(jnp.float32)
        + kv_z[0].astype(jnp.float32)
        + kv_z[1].astype(jnp.float32)
        + kv_z[2].astype(jnp.float32)
    )

    back_out.wait_send()
    kv_over_y.wait_send()
    kv_over_c.wait_send()
    kv_over_x.wait_send()
    for kind in range(3):
        f_x_own(kind).wait()
    for index in range(len(tasks)):
        f_x(index).wait_send()
    for step in range(1, z_size):
        for kind in range(3):
            f_z(step, kind).wait()
    for copy in gain_hops + gain_last + kv_over_z:
        copy.wait_send()
    for step in range(z_size):
        mix_over_y(step).wait_send()
        if step:
            mix_over_z(step).wait_send()
        for kind in range(2):
            w_c(kind, step, 0).wait_send()
            w_c(kind, step, 1).wait_send()
            w_x(kind, step).wait_send()
            if step:
                w_z(kind, step).wait_send()


def post_call(
    grad_normed,
    mid,
    tokens,
    cotangent,
    gains,
    normed_one,
    rotated,
    keys,
    values,
    attn_vals,
    table,
    allowed,
    kv_weight,
    query_weight,
    out_weight,
    mix_parts,
    ffn_sums,
):
    z_size = lax.axis_size("z")
    own, width = tokens.shape
    seq = 2 * own
    head = keys.shape[1]
    cols = attn_vals.shape[1]
    rows = width // (4 * z_size)
    units = ffn_sums.shape[4]
    low = lambda *dims: pltpu.VMEM(dims, jnp.bfloat16)
    full = lambda *dims: pltpu.VMEM(dims, jnp.float32)
    out_full = lambda *dims: jax.ShapeDtypeStruct(dims, jnp.float32)
    out_low = lambda *dims: jax.ShapeDtypeStruct(dims, jnp.bfloat16)
    dma = lambda *lead: pltpu.SemaphoreType.DMA(lead)
    vmem = pl.BlockSpec(memory_space=pltpu.VMEM)
    hbm = pl.BlockSpec(memory_space=pl.ANY)
    z = z_size
    return pl.pallas_call(
        functools.partial(post_kernel, z_size),
        out_shape=(
            out_low(own, width),
            out_low(own, width),
            out_full(8, width // z),
            out_full(rows // 2, 2 * head),
            out_full(rows, cols),
            out_full(rows, cols),
            out_low(3, z, rows, units),
        ),
        in_specs=[vmem] * 11 + [hbm] * 6,
        out_specs=(vmem,) * 6 + (hbm,),
        scratch_shapes=[
            low(z, 2, 2, 2, rows // 2, 2 * head),
            low(width, cols),
            low(width, cols),
            low(width, cols),
            low(seq, width),
            full(own, width),
            low(seq, cols),
            low(seq, 2 * head),
            full(2, seq, head),
            low(own, width),
            low(z, width, own),
            low(z - 1, width, own),
            low(z, width, own),
            low(z, 2, rows, cols),
            low(z, rows, cols),
            low(z + 1, rows, cols),
            low(z, 2, rows, cols),
            low(z, rows, cols),
            low(z + 1, rows, cols),
            low(z, 2, 2, rows // 2, 2 * head),
            low(z, 2, rows // 2, 2 * head),
            low(z, rows // 2, 2 * head),
            low(z - 1, rows // 2, 2 * head),
            full(4, 8, width // z),
            full(6, 8, width // z),
            low(6, rows, units),
            low(2, rows, units),
            dma(4 + z),
            dma(2),
            dma(9),
            dma(9),
            dma(3, z),
            dma(3, z),
            dma(3),
            dma(3),
            dma(z),
            dma(z),
            dma(z),
            dma(z),
            dma(2, z, 2),
            dma(2, z, 2),
            dma(2, z),
            dma(2, z),
            dma(2, z),
            dma(2, z + 1),
            dma(2),
            dma(2),
            dma(z),
            dma(z),
            dma(6),
            dma(6),
        ],
        compiler_params=pltpu.CompilerParams(
            collective_id=2, has_side_effects=True, vmem_limit_bytes=VMEM_BYTES
        ),
        cost_estimate=pl.CostEstimate(
            flops=14 * seq * width * cols,
            bytes_accessed=10 * width * cols,
            transcendentals=seq * seq * cols // head,
        ),
    )(
        mid,
        tokens,
        cotangent,
        gains,
        normed_one,
        rotated,
        keys,
        values,
        attn_vals,
        table,
        allowed,
        kv_weight.reshape(z, 2, 2, 2, rows // 2, kv_weight.shape[1]),
        query_weight,
        out_weight,
        mix_parts,
        grad_normed,
        ffn_sums,
    )


def layout_kernel(
    z_size,
    main,
    sum_ref,
    ffn_ref,
    q_ref,
    o_ref,
    kv_ref,
    mixed_in,
    tgrad_in,
    wg_ref,
    wu_ref,
    wd_ref,
    qg_ref,
    og_ref,
    kvg_ref,
    mixed_ref,
    tgrad_ref,
):
    me_z = lax.axis_index("z")
    for kind, out in enumerate((wg_ref, wu_ref, wd_ref)):
        out[:, z_size * main :] = jnp.zeros((out.shape[0], 64 * z_size), jnp.float32)
        for step in range(z_size):
            at = lax.rem(me_z - step + z_size, z_size)
            values = ffn_ref[kind, step].astype(jnp.float32)
            if step == 0:
                values = values + sum_ref[kind, 0, 0].astype(jnp.float32)
            body = pl.ds(pl.multiple_of(at * main, 128), main)
            out[:, body] = values[:, :main]
            tail = pl.ds(pl.multiple_of(z_size * main + at // 2 * 128, 128), 128)
            out[:, tail] += values[:, main:]
    qg_ref[...] = q_ref[...]
    og_ref[...] = o_ref[...]
    kvg_ref[...] = kv_ref[...]
    mixed_ref[...] = mixed_in[...]
    tgrad_ref[...] = tgrad_in[...]


def layout_call(ffn_sums, ffn_grads, query_grad, out_grad, kv_grad, mixed, tokens_grad, ffn_cols):
    z_size = lax.axis_size("z")
    main, units = ragged_split(ffn_cols, z_size)
    rows, cols = query_grad.shape
    parts = rows // 32
    kv_rows = kv_grad.shape[0] // parts
    full = lambda *dims: jax.ShapeDtypeStruct(dims, jnp.float32)
    row = lambda height, width: pl.BlockSpec((height, width), lambda index: (index, 0))
    own, width = mixed.shape
    share = pl.BlockSpec((own, width // parts), lambda index: (0, index))
    specs = [row(32, cols), row(32, cols), row(kv_rows, kv_grad.shape[1]), share, share]
    return pl.pallas_call(
        functools.partial(layout_kernel, z_size, main),
        grid=(parts,),
        out_shape=(
            *[full(rows, ffn_cols)] * 3,
            full(rows, cols),
            full(rows, cols),
            full(*kv_grad.shape),
            jax.ShapeDtypeStruct(mixed.shape, jnp.bfloat16),
            jax.ShapeDtypeStruct(mixed.shape, jnp.bfloat16),
        ),
        in_specs=[
            pl.BlockSpec((3, 1, 1, 32, units), lambda index: (0, 0, 0, index, 0)),
            pl.BlockSpec((3, z_size, 32, units), lambda index: (0, 0, index, 0)),
            *specs,
        ],
        out_specs=(*[row(32, ffn_cols)] * 3, *specs),
        compiler_params=pltpu.CompilerParams(vmem_limit_bytes=VMEM_BYTES),
    )(ffn_sums, ffn_grads, query_grad, out_grad, kv_grad, mixed, tokens_grad)


FF_SPLIT = 4


def ffn_pass(normed, grad_out, gate_weight, up_weight, down_weight):
    gate = jnp.dot(normed, gate_weight, preferred_element_type=jnp.float32)
    up_proj = jnp.dot(normed, up_weight, preferred_element_type=jnp.float32)
    grad_hidden = jnp.dot(grad_out, down_weight, preferred_element_type=jnp.float32)
    product, pull = jax.vjp(gelu_product, gate, up_proj)
    hidden = product.astype(jnp.bfloat16)
    grad_gate_f, grad_up_f = pull(grad_hidden)
    grad_gate = grad_gate_f.astype(jnp.bfloat16)
    grad_up = grad_up_f.astype(jnp.bfloat16)
    mixed_part = matmul_nt(hidden, down_weight).astype(jnp.bfloat16)
    normed_part = (matmul_nt(grad_gate, gate_weight) + matmul_nt(grad_up, up_weight)).astype(
        jnp.bfloat16
    )
    weight_parts = [
        matmul_tn(normed, grad_gate).astype(jnp.bfloat16),
        matmul_tn(normed, grad_up).astype(jnp.bfloat16),
        matmul_tn(grad_out, hidden).astype(jnp.bfloat16),
    ]
    return mixed_part, normed_part, weight_parts


def shards_general(
    tokens,
    segments,
    positions,
    cotangent,
    attn_gain,
    ffn_gain,
    w_kv,
    w_query,
    w_out,
    w_gate,
    w_up,
    w_down,
):
    everywhere = ("z", "xc", "mp")
    dp = ("z", "xc")
    z_size = lax.axis_size("z")
    xc_size = lax.axis_size("xc")
    gains = lax.all_gather(
        jnp.stack([attn_gain, ffn_gain], axis=1), everywhere, axis=0, tiled=True
    ).astype(jnp.float32)
    gain_one, gain_two = gains[:, 0], gains[:, 1]
    kv_weight = lax.all_gather(w_kv, everywhere, axis=0, tiled=True)
    head_dim = kv_weight.shape[1] // 2
    width = tokens.shape[1]
    seq_len = segments.shape[0]
    heads_here = w_query.shape[1] // head_dim
    scale = head_dim ** (-0.5)
    cosine, sine = rotary_angles(positions, head_dim)
    inputs_f = tokens.astype(jnp.float32)
    tokens_all = lax.all_gather(tokens, "mp", axis=0, tiled=True)
    normed_one = norm_gain(tokens_all.astype(jnp.float32), gain_one).astype(jnp.bfloat16)
    query_weight = lax.all_gather(w_query, dp, axis=0, tiled=True)
    out_weight = lax.all_gather(w_out, dp, axis=0, tiled=True)

    rows = w_gate.shape[0]
    unit = w_gate.shape[1] // z_size

    def spread(weight):
        pieces = weight.reshape(rows, z_size, unit).transpose(1, 0, 2)
        pieces = lax.all_to_all(pieces, "z", split_axis=0, concat_axis=0, tiled=True)
        return lax.all_gather(pieces, "xc", axis=1, tiled=False).reshape(width, unit)

    gate_weight, up_weight, down_weight = spread(w_gate), spread(w_up), spread(w_down)
    grad_all = lax.all_gather(cotangent, ("z", "mp"), axis=0, tiled=True)

    query = jnp.dot(normed_one, query_weight, preferred_element_type=jnp.float32).reshape(
        seq_len, heads_here, head_dim
    )
    rotated = (rotate(query, cosine[:, None], sine[:, None]) * scale).astype(jnp.bfloat16)
    keyval = jnp.dot(normed_one, kv_weight, preferred_element_type=jnp.float32)
    keys = rotate(keyval[:, :head_dim], cosine, sine).astype(jnp.bfloat16)
    values = keyval[:, head_dim:].astype(jnp.bfloat16)
    allowed = block_allowed(segments, 0, seq_len)
    scores = jnp.einsum("thd,sd->hts", rotated, keys, preferred_element_type=jnp.float32)
    scores = jnp.where(allowed[None], scores, masked_score)
    row_max = jnp.max(scores, axis=-1, keepdims=True)
    weights = jnp.exp(scores - row_max)
    probs = weights / jnp.sum(weights, axis=-1, keepdims=True)
    probs_low = probs.astype(jnp.bfloat16)
    attn_vals = (
        jnp.einsum("hts,sd->thd", probs_low, values, preferred_element_type=jnp.float32)
        .reshape(seq_len, heads_here * head_dim)
        .astype(jnp.bfloat16)
    )
    mid = inputs_f + lax.psum_scatter(
        matmul_nt(attn_vals, out_weight).astype(jnp.bfloat16),
        "mp",
        scatter_dimension=0,
        tiled=True,
    ).astype(jnp.float32)
    normed_two = norm_gain(mid, gain_two).astype(jnp.bfloat16)
    normed_all = lax.all_gather(normed_two, ("z", "mp"), axis=0, tiled=True)

    mixed_part, normed_part, weight_parts = ffn_pass(
        normed_all, grad_all, gate_weight, up_weight, down_weight
    )
    grad_normed_two = lax.psum_scatter(
        normed_part, ("z", "mp"), scatter_dimension=0, tiled=True
    ).astype(jnp.float32)
    mixed = (
        mid
        + lax.psum_scatter(mixed_part, ("z", "mp"), scatter_dimension=0, tiled=True).astype(
            jnp.float32
        )
    ).astype(jnp.bfloat16)

    def collect(part):
        pieces = part.reshape(z_size, xc_size, rows, unit).transpose(1, 0, 2, 3)
        pieces = pieces.reshape(xc_size * z_size * rows, unit)
        pieces = lax.psum_scatter(pieces, "xc", scatter_dimension=0, tiled=True)
        pieces = pieces.reshape(z_size, rows, unit)
        pieces = lax.all_to_all(pieces, "z", split_axis=0, concat_axis=0, tiled=True)
        return pieces.transpose(1, 0, 2).reshape(rows, z_size * unit).astype(jnp.float32)

    w_gate_grad, w_up_grad, w_down_grad = [collect(part) for part in weight_parts]

    norm_pull_two = jax.vjp(norm_gain, mid, gain_two)[1]
    grad_mid_norm, grad_gain_two = norm_pull_two(grad_normed_two)
    grad_mid = cotangent.astype(jnp.float32) + grad_mid_norm
    grad_mid_all = lax.all_gather(grad_mid.astype(jnp.bfloat16), "mp", axis=0, tiled=True)
    grad_vals = (
        jnp.dot(grad_mid_all, out_weight, preferred_element_type=jnp.float32)
        .astype(jnp.bfloat16)
        .reshape(seq_len, heads_here, head_dim)
    )
    grad_probs = jnp.einsum("thd,sd->hts", grad_vals, values, preferred_element_type=jnp.float32)
    delta = jnp.sum(probs * grad_probs, axis=-1, keepdims=True)
    grad_scores = (probs * (grad_probs - delta)).astype(jnp.bfloat16)
    grad_rot = jnp.einsum("hts,sd->thd", grad_scores, keys, preferred_element_type=jnp.float32)
    key_sum = jnp.einsum("hts,thd->sd", grad_scores, rotated, preferred_element_type=jnp.float32)
    value_sum = jnp.einsum("hts,thd->sd", probs_low, grad_vals, preferred_element_type=jnp.float32)
    grad_query = (
        (unrotate(grad_rot, cosine[:, None], sine[:, None]) * scale)
        .reshape(seq_len, heads_here * head_dim)
        .astype(jnp.bfloat16)
    )
    grad_kv = jnp.concatenate([unrotate(key_sum, cosine, sine), value_sum], axis=1).astype(
        jnp.bfloat16
    )
    grad_normed_one = lax.psum_scatter(
        (matmul_nt(grad_query, query_weight) + matmul_nt(grad_kv, kv_weight)).astype(jnp.bfloat16),
        "mp",
        scatter_dimension=0,
        tiled=True,
    ).astype(jnp.float32)
    norm_pull_one = jax.vjp(norm_gain, inputs_f, gain_one)[1]
    grad_input_norm, grad_gain_one = norm_pull_one(grad_normed_one)
    tokens_grad = (grad_mid + grad_input_norm).astype(jnp.bfloat16)

    w_query_grad = lax.psum_scatter(
        matmul_tn(normed_one, grad_query).astype(jnp.bfloat16), dp, scatter_dimension=0, tiled=True
    ).astype(jnp.float32)
    w_out_grad = lax.psum_scatter(
        matmul_tn(grad_mid_all, attn_vals).astype(jnp.bfloat16), dp, scatter_dimension=0, tiled=True
    ).astype(jnp.float32)
    small = jnp.concatenate(
        [matmul_tn(normed_one, grad_kv), grad_gain_one[:, None], grad_gain_two[:, None]], axis=1
    )
    small = lax.psum_scatter(small, everywhere, scatter_dimension=0, tiled=True)
    kv_grad = small[:, : 2 * head_dim]
    return (
        mixed,
        tokens_grad,
        small[:, 2 * head_dim],
        small[:, 2 * head_dim + 1],
        kv_grad,
        w_query_grad,
        w_out_grad,
        w_gate_grad,
        w_up_grad,
        w_down_grad,
    )


def shards_fast(
    tokens,
    segments,
    positions,
    cotangent,
    attn_gain,
    ffn_gain,
    w_kv,
    w_query,
    w_out,
    w_gate,
    w_up,
    w_down,
):
    seq_len = segments.shape[0]
    cosine, sine = rotary_angles(positions, w_kv.shape[1] // 2)
    table = jnp.stack(
        [
            jnp.concatenate([cosine, cosine], axis=1),
            jnp.concatenate([-sine, sine], axis=1),
        ]
    )
    gain_rows = jnp.pad(
        jnp.stack([attn_gain, ffn_gain]).astype(jnp.float32),
        ((0, 6), (0, 128 - attn_gain.shape[0])),
    )
    segment_rows = jnp.broadcast_to(segments.astype(jnp.float32)[None, :], (8, seq_len))
    (
        normed_one,
        rotated,
        keys,
        values,
        attn_vals,
        mid,
        normed_two,
        gains,
        allowed,
        kv_weight,
        query_weight,
        out_weight,
        ffn_weights,
        grad_all,
    ) = pre_call(
        tokens,
        w_kv,
        gain_rows,
        table,
        segment_rows,
        cotangent,
        w_query,
        w_out,
        (w_gate, w_up, w_down),
    )
    main = ragged_split(w_gate.shape[1], lax.axis_size("z"))[0]
    grad_normed_two, mix_parts, ffn_sums = ffn_call(
        normed_two, grad_all, ffn_weights, w_gate.shape[0], main
    )
    mixed, tokens_grad, gain_grads, kv_grad, query_grad, out_grad, ffn_grads = post_call(
        grad_normed_two,
        mid,
        tokens,
        cotangent,
        gains,
        normed_one,
        rotated,
        keys,
        values,
        attn_vals,
        table,
        allowed,
        kv_weight,
        query_weight,
        out_weight,
        mix_parts,
        ffn_sums,
    )
    *ffn_out, query_grad, out_grad, kv_grad, mixed, tokens_grad = layout_call(
        ffn_sums,
        ffn_grads,
        query_grad,
        out_grad,
        kv_grad,
        mixed,
        tokens_grad,
        w_gate.shape[1],
    )
    share = attn_gain.shape[0]
    place = lax.axis_index(("z", "x", "c", "mp")) * share
    gain_grads = gain_grads.reshape(2, gain_grads.size // 2)
    gain_grads = lax.dynamic_slice(gain_grads, (0, place), (2, share))
    return (
        mixed,
        tokens_grad,
        gain_grads[0],
        gain_grads[1],
        kv_grad,
        query_grad,
        out_grad,
        *ffn_out,
    )


def solution(mesh):
    dp_size, mp_size = mesh.shape["dp"], mesh.shape["mp"]
    if dp_size == 4 * FF_SPLIT and mp_size == 2:
        body, dp = shards_fast, ("z", "x", "c")
        sizes = (FF_SPLIT, 2, 2, mp_size)
    else:
        body, dp = shards_general, ("z", "xc")
        sizes = (FF_SPLIT, dp_size // FF_SPLIT, mp_size)
    all_axes = (*dp, "mp")
    fine = jax.sharding.Mesh(mesh.devices.reshape(sizes), all_axes)
    in_specs = (
        P(all_axes, None),
        P(dp),
        P(dp),
        P(all_axes, None),
        P(all_axes),
        P(all_axes),
        P(all_axes, None),
        P(dp, "mp"),
        P(dp, "mp"),
        P(dp, "mp"),
        P(dp, "mp"),
        P(dp, "mp"),
    )
    out_specs = (
        P(all_axes, None),
        P(all_axes, None),
        P(all_axes),
        P(all_axes),
        P(all_axes, None),
        P(dp, "mp"),
        P(dp, "mp"),
        P(dp, "mp"),
        P(dp, "mp"),
        P(dp, "mp"),
    )
    return jax.shard_map(body, mesh=fine, in_specs=in_specs, out_specs=out_specs, check_vma=False)
```

```python
import functools

import jax
import jax.numpy as jnp
from jax import lax
from jax.experimental import pallas as pl
from jax.experimental.pallas import tpu as pltpu
from jax.sharding import PartitionSpec as P

WINDOW = 2048


epsilon = 1e-06
rope_base = 10000.0
masked_score = -1e30
VMEM_BYTES = 66_000_000


def norm_gain(values, gain):
    return values * lax.rsqrt(jnp.mean(values * values, axis=-1, keepdims=True) + epsilon) * gain


def rotary_angles(positions, head_width):
    quarter = head_width // 4
    freqs = rope_base ** (-jnp.arange(quarter).astype(jnp.float32) / quarter)
    phase = positions.astype(jnp.float32)[:, None] * freqs[None, :]
    return (jnp.cos(phase), jnp.sin(phase))


def rotate(values, cosine, sine):
    quarter = cosine.shape[-1]
    first_half = values[..., :quarter]
    second_half = values[..., quarter : 2 * quarter]
    return jnp.concatenate(
        [
            first_half * cosine - second_half * sine,
            second_half * cosine + first_half * sine,
            values[..., 2 * quarter :],
        ],
        axis=-1,
    )


def unrotate(values, cosine, sine):
    quarter = cosine.shape[-1]
    first_half = values[..., :quarter]
    second_half = values[..., quarter : 2 * quarter]
    return jnp.concatenate(
        [
            first_half * cosine + second_half * sine,
            second_half * cosine - first_half * sine,
            values[..., 2 * quarter :],
        ],
        axis=-1,
    )


def gelu_product(gate, up_proj):
    return jax.nn.gelu(gate, approximate=True) * up_proj


def matmul_nt(left, right):
    return lax.dot_general(
        left, right, (((1,), (1,)), ((), ())), preferred_element_type=jnp.float32
    )


def matmul_tn(left, right):
    return lax.dot_general(
        left, right, (((0,), (0,)), ((), ())), preferred_element_type=jnp.float32
    )


def block_allowed(segments, first_row, rows):
    seq_len = segments.shape[0]
    query_rows = first_row + jnp.arange(rows)
    key_rows = jnp.arange(seq_len)
    return (
        (segments[:, None] == segments[None, :])
        & (key_rows[None, :] <= query_rows[:, None])
        & (query_rows[:, None] - key_rows[None, :] < WINDOW)
    )


MESH_ID = pl.DeviceIdType.MESH
GELU_A = 0.7978845608028654
GELU_B = 0.044715
TILE = 256
WIDE = 512


def remote(src, dst, send_sem, recv_sem, where):
    return pltpu.make_async_remote_copy(
        src_ref=src,
        dst_ref=dst,
        send_sem=send_sem,
        recv_sem=recv_sem,
        device_id=where,
        device_id_type=MESH_ID,
    )


def dot_nn(left, right):
    return lax.dot_general(
        left, right, (((1,), (0,)), ((), ())), preferred_element_type=jnp.float32
    )


def gelu_parts(gate):
    square = gate * gate
    bend = jnp.tanh(GELU_A * gate * (1.0 + GELU_B * square))
    half = 0.5 * (1.0 + bend)
    slope = half + 0.5 * gate * (1.0 - bend * bend) * GELU_A * (1.0 + 3.0 * GELU_B * square)
    return gate * half, slope


def add_rows(first, rest, out, count):
    def body(index, carry):
        step = pl.ds(pl.multiple_of(index * 32, 32), 32)
        total = first[step, :].astype(jnp.float32)
        for other in rest:
            total = total + other[step, :].astype(jnp.float32)
        out[step, :] = total.astype(out.dtype)
        return carry

    lax.fori_loop(0, count // 32, body, 0)


def norm_back(values, gain, upstream):
    scale = lax.rsqrt(jnp.mean(values * values, axis=-1, keepdims=True) + epsilon)
    normed = values * scale
    pulled = gain * upstream
    back = scale * (pulled - normed * jnp.mean(normed * pulled, axis=-1, keepdims=True))
    return back, jnp.sum(upstream * normed, axis=0, keepdims=True)


def ffn_kernel(
    z_size,
    main,
    gain_ref,
    own_hbm,
    dy_hbm,
    w_hbm,
    mid_hbm,
    gm_ref,
    gain_part,
    mix_hbm,
    sums_hbm,
    gm_hbm,
    n2,
    dy,
    w3,
    h3,
    n2_t,
    dy_t,
    gn_part,
    mix_buf,
    gn_y,
    gn_z,
    gn_s,
    c_in,
    x_in,
    mid,
    load_sem,
    mix_sem,
    ag_y_send,
    ag_y_recv,
    ag_z_send,
    ag_z_recv,
    rs_y_send,
    rs_y_recv,
    rs_z_send,
    rs_z_recv,
    c_send,
    c_recv,
    x_send,
    x_recv,
    out_sem,
):
    own = own_hbm.shape[0] // 2
    width = own_hbm.shape[1]
    units = w3.shape[2]
    rows = c_in.shape[3]
    span = width // z_size
    me_y, me_z = lax.axis_index("mp"), lax.axis_index("z")
    me_x, me_c = lax.axis_index("x"), lax.axis_index("c")
    mine = pl.ds(pl.multiple_of(me_y * own, own), own)
    theirs = pl.ds(pl.multiple_of((1 - me_y) * own, own), own)
    to_y, to_x, to_c = {"mp": 1 - me_y}, {"x": 1 - me_x}, {"c": 1 - me_c}

    def ahead(step):
        return lax.rem(me_z + step, z_size)

    def to_z(step):
        return {"z": ahead(step)}

    def row_block(z_at, x_at, c_at):
        return pl.ds(pl.multiple_of(((z_at * 2 + x_at) * 2 + c_at) * rows, rows), rows)

    inner = (me_z > 0) & (me_z < z_size - 1)
    outer = (me_z == 0) | (me_z == z_size - 1)

    def w_load(index, columns):
        cols = pl.ds(0, columns)
        return pltpu.make_async_copy(
            w_hbm.at[index, :, cols], w3.at[index, :, cols], load_sem.at[z_size + index]
        )

    def w_loads(act):
        for case, columns in ((inner, units), (outer, main)):

            @pl.when(case)
            def _(columns=columns):
                for index in range(3):
                    act(w_load(index, columns))

    w_loads(lambda copy: copy.start())
    dy_loads = [
        pltpu.make_async_copy(dy_hbm.at[index], dy, load_sem.at[index])
        for index in range(z_size)
    ]
    own_load = pltpu.make_async_copy(own_hbm, n2.at[0], load_sem.at[z_size + 3])
    mid_load = pltpu.make_async_copy(mid_hbm, mid, load_sem.at[z_size + 4])
    for load in (own_load, dy_loads[0], mid_load):
        load.start()

    barrier = pltpu.get_barrier_semaphore()
    peers = [to_y, to_x, to_c] + [to_z(step) for step in range(1, z_size)]
    for where in peers:
        pl.semaphore_signal(barrier, inc=1, device_id=where, device_id_type=MESH_ID)
    pl.semaphore_wait(barrier, len(peers))

    def ag_y(index):
        block = n2.at[index, mine]
        return remote(block, block, ag_y_send.at[index], ag_y_recv.at[index], to_y)

    def ag_y_in(index):
        block = n2.at[index, theirs]
        return remote(block, block, ag_y_send.at[index], ag_y_recv.at[index], to_y)

    def ag_z(index):
        src = own_hbm.at[mine] if index == 0 else n2.at[index, mine]
        return remote(
            src, n2.at[index + 1, mine], ag_z_send.at[index], ag_z_recv.at[index + 1], to_z(1)
        )

    def ag_z_in(index):
        block = n2.at[index, mine]
        return remote(block, block, ag_z_send.at[0], ag_z_recv.at[index], to_z(1))

    def ag_last():
        return remote(
            n2.at[2, theirs], n2.at[3, theirs], ag_y_send.at[3], ag_y_recv.at[3], to_z(1)
        )

    def forward(index):
        ag_z_in(index).wait_recv()
        ag_z(index).start()
        ag_y(index).start()

    ag_z(0).start()

    mix_copies = []

    def turn(source, target, index):
        def turn_tile(tile, carry):
            at = pl.ds(pl.multiple_of(tile * span, 128), span)
            target[at, pl.ds(index * 2 * own, 2 * own)] = source[:, at].T
            return carry

        lax.fori_loop(0, z_size, turn_tile, 0)

    def chunk(index):
        if index:
            mix_copies[index - 1].wait()
        dy_loads[index].wait()
        rows_at = pl.ds(index * 2 * own, 2 * own)

        def up_tile(tile, carry):
            cols = pl.ds(pl.multiple_of(tile * TILE, TILE), TILE)
            gate = dot_nn(n2[index], w3[0, :, cols])
            up_proj = dot_nn(n2[index], w3[1, :, cols])
            grad_hidden = dot_nn(dy[...], w3[2, :, cols])
            act, slope = gelu_parts(gate)
            h3[0, rows_at, cols] = (grad_hidden * up_proj * slope).astype(jnp.bfloat16)
            h3[1, rows_at, cols] = (grad_hidden * act).astype(jnp.bfloat16)
            h3[2, rows_at, cols] = (act * up_proj).astype(jnp.bfloat16)
            return carry

        lax.fori_loop(0, units // TILE, up_tile, 0)

        def down_tile(tile, carry):
            at = pl.ds(pl.multiple_of(tile * span, 128), span)
            normed = matmul_nt(w3[0, at, :], h3[0, rows_at, :]) + matmul_nt(
                w3[1, at, :], h3[1, rows_at, :]
            )
            mixed = matmul_nt(w3[2, at, :], h3[2, rows_at, :])
            for half in range(2):
                cols = slice(half * own, (half + 1) * own)
                gn_part[index, half, at, :] = normed[:, cols].astype(jnp.bfloat16)
                mix_buf[half, at, :] = mixed[:, cols].astype(jnp.bfloat16)
            return carry

        lax.fori_loop(0, z_size, down_tile, 0)
        copy = pltpu.make_async_copy(mix_buf, mix_hbm.at[index], mix_sem.at[index])
        copy.start()
        mix_copies.append(copy)
        if index:
            rs_y(index).start()
        turn(n2.at[index], n2_t, index)
        turn(dy, dy_t, index)
        if index + 1 < z_size:
            dy_loads[index + 1].start()

    def rs_y(index):
        return remote(
            gn_part.at[index, 1 - me_y], gn_y.at[index], rs_y_send.at[index], rs_y_recv.at[index], to_y
        )

    def rs_z(index):
        return remote(
            gn_s.at[index - 1],
            gn_z.at[index - 1],
            rs_z_send.at[index],
            rs_z_recv.at[index - 1],
            to_z(1),
        )

    def rs_step(index):
        rs_y(index).wait_recv()
        slot = (index - 2) % z_size
        if index != 1:
            remote(
                gn_s.at[slot], gn_z.at[slot], rs_z_send.at[1], rs_z_recv.at[slot], to_z(1)
            ).wait_recv()

        def add_tile(tile, carry):
            at = pl.ds(pl.multiple_of(tile * TILE, TILE), TILE)
            total = gn_part[index, me_y, at, :].astype(jnp.float32) + gn_y[index, at, :].astype(
                jnp.float32
            )
            if index != 1:
                total = total + gn_z[slot, at, :].astype(jnp.float32)
            if index == 0:
                gm_ref[:, at] = total.T
            else:
                gn_s[index - 1, at, :] = total.astype(jnp.bfloat16)
            return carry

        lax.fori_loop(0, width // TILE, add_tile, 0)
        if index != 0:
            rs_z(index).start()


    def grads(step):
        at = pl.ds(pl.multiple_of(ahead(step) * span, 128), span)
        for kind, source in enumerate((n2_t, n2_t, dy_t)):

            def tile_body(tile, carry, kind=kind, source=source):
                cols = pl.ds(pl.multiple_of(tile * WIDE, WIDE), WIDE)
                w3[kind, at, cols] = dot_nn(source[at, :], h3[kind, :, cols]).astype(jnp.bfloat16)
                return carry

            lax.fori_loop(0, units // WIDE, tile_body, 0)
        for far in (1, 0):
            for kind in range(3):
                over_c(kind, step, far).start()

    def over_c(kind, step, far):
        x_at = 1 - me_x if far else me_x
        return remote(
            w3.at[kind, row_block(ahead(step), x_at, 1 - me_c)],
            c_in.at[kind, step, far],
            c_send.at[kind, step, far],
            c_recv.at[kind, step, far],
            to_c,
        )

    def over_x(kind):
        return remote(
            w3.at[kind, row_block(ahead(1), 1 - me_x, me_c)],
            x_in.at[kind],
            x_send.at[kind],
            x_recv.at[kind],
            to_x,
        )

    out_copies = []

    def keep(kind, step, far, block):
        copy = pltpu.make_async_copy(
            block, sums_hbm.at[kind, step, far], out_sem.at[kind, step, far]
        )
        copy.start()
        out_copies.append(copy)

    def core_sums(step):
        for far in (1, 0):
            for kind in range(3):
                over_c(kind, step, far).wait_recv()
                x_at = 1 - me_x if far else me_x
                block = w3.at[kind, row_block(ahead(step), x_at, me_c)]
                add_rows(block, [c_in.at[kind, step, far]], block, rows)
                if step != 1:
                    keep(kind, step, far, block)
                elif far:
                    over_x(kind).start()

    def first_sums():
        for kind in range(3):
            over_x(kind).wait_recv()
            block = w3.at[kind, row_block(ahead(1), me_x, me_c)]
            add_rows(block, [x_in.at[kind]], block, rows)
            keep(kind, 1, 0, block)

    own_load.wait()
    w_loads(lambda copy: copy.wait())

    @pl.when(outer)
    def _():
        w3[:, :, main:] = jnp.zeros((3, width, units - main), jnp.bfloat16)

    chunk(0)
    forward(1)
    forward(2)
    ag_y_in(1).wait_recv()
    chunk(1)
    ag_y_in(2).wait_recv()
    ag_last().start()
    chunk(2)
    rs_step(1)
    ag_z_in(3).wait_recv()
    ag_last().wait_recv()
    chunk(3)
    rs_y(0).start()
    rs_step(2)
    grads(1)
    grads(2)
    core_sums(1)
    rs_step(3)
    grads(3)
    core_sums(2)
    grads(0)
    core_sums(3)
    rs_step(0)
    core_sums(0)

    cot_load = pltpu.make_async_copy(
        dy_hbm.at[0, mine], dy.at[pl.ds(0, own)], load_sem.at[z_size + 3]
    )
    cot_load.start()
    cot_load.wait()
    mid_load.wait()

    def mid_rows(index, total):
        at = pl.ds(pl.multiple_of(index * 32, 32), 32)
        grad, gain_sum = norm_back(mid[at, :], gain_ref[1:2, :], gm_ref[at, :])
        grad = grad + dy[at, :].astype(jnp.float32)
        gm_ref[at, :] = grad
        dy[pl.ds(pl.multiple_of(own + index * 32, 32), 32), :] = grad.astype(jnp.bfloat16)
        return total + gain_sum

    gain_sum = lax.fori_loop(0, own // 32, mid_rows, jnp.zeros((1, width), jnp.float32))
    gm_save = pltpu.make_async_copy(dy.at[pl.ds(own, own)], gm_hbm, load_sem.at[z_size + 3])
    gm_save.start()
    for index in range(4):
        gain_part[index : index + 1, :] = jnp.zeros((1, span), jnp.float32)
        gain_part[4 + index : 5 + index, :] = gain_sum[:, index * span : (index + 1) * span]
    first_sums()
    gm_save.wait()

    for copy in mix_copies[3:] + out_copies:
        copy.wait()
    for index in range(z_size):
        if index in (1, 2):
            ag_y(index).wait_send()
        if index == 3:
            ag_last().wait_send()
        rs_y(index).wait_send()
        if index < z_size - 1:
            ag_z(index).wait_send()
        if index:
            rs_z(index).wait_send()
        for kind in range(3):
            over_c(kind, index, 0).wait_send()
            over_c(kind, index, 1).wait_send()
            if index == 1:
                over_x(kind).wait_send()


def ffn_call(gains, normed, grad_all, weights, mid, rows, main):
    z_size = lax.axis_size("z")
    pair, width = normed.shape
    units = weights.shape[2]
    own = pair // 2
    wide = lambda *lead: pltpu.VMEM((*lead, width), jnp.bfloat16)
    tall = lambda *lead: pltpu.VMEM((*lead, width, own), jnp.bfloat16)
    dma = lambda *lead: pltpu.SemaphoreType.DMA(lead)
    vmem = pl.BlockSpec(memory_space=pltpu.VMEM)
    hbm = pl.BlockSpec(memory_space=pl.ANY)
    return pl.pallas_call(
        functools.partial(ffn_kernel, z_size, main),
        out_shape=(
            jax.ShapeDtypeStruct((own, width), jnp.float32),
            jax.ShapeDtypeStruct((8, width // z_size), jnp.float32),
            jax.ShapeDtypeStruct((z_size, 2, width, own), jnp.bfloat16),
            jax.ShapeDtypeStruct((3, z_size, 2, rows, units), jnp.bfloat16),
            jax.ShapeDtypeStruct((own, width), jnp.bfloat16),
        ),
        in_specs=[vmem, hbm, hbm, hbm, hbm],
        out_specs=(vmem, vmem, hbm, hbm, hbm),
        scratch_shapes=[
            wide(z_size, pair),
            wide(pair),
            pltpu.VMEM(weights.shape, jnp.bfloat16),
            pltpu.VMEM((3, z_size * pair, units), jnp.bfloat16),
            pltpu.VMEM((width, z_size * pair), jnp.bfloat16),
            pltpu.VMEM((width, z_size * pair), jnp.bfloat16),
            tall(z_size, 2),
            tall(2),
            tall(z_size),
            tall(z_size - 1),
            tall(z_size - 1),
            pltpu.VMEM((3, z_size, 2, rows, units), jnp.bfloat16),
            pltpu.VMEM((3, rows, units), jnp.bfloat16),
            pltpu.VMEM((own, width), jnp.float32),
            dma(z_size + 5),
            dma(z_size),
            dma(z_size),
            dma(z_size),
            dma(z_size),
            dma(z_size),
            dma(z_size),
            dma(z_size),
            dma(z_size),
            dma(z_size),
            dma(3, z_size, 2),
            dma(3, z_size, 2),
            dma(3),
            dma(3),
            dma(3, z_size, 2),
        ],
        compiler_params=pltpu.CompilerParams(
            collective_id=0, has_side_effects=True, vmem_limit_bytes=VMEM_BYTES
        ),
        cost_estimate=pl.CostEstimate(
            flops=18 * z_size * pair * width * units,
            bytes_accessed=4 * weights.size + 12 * z_size * pair * width,
            transcendentals=z_size * pair * units,
        ),
    )(gains, normed, grad_all, weights, mid)


def spin(values, table):
    first = values[:, : values.shape[1] // 2]
    turned = first * table[0] + pltpu.roll(first, first.shape[1] // 2, 1) * table[1]
    return jnp.concatenate([turned, values[:, values.shape[1] // 2 :]], axis=1)


def spin_back(values, table):
    first = values[:, : values.shape[1] // 2]
    turned = first * table[0] - pltpu.roll(first, first.shape[1] // 2, 1) * table[1]
    return jnp.concatenate([turned, values[:, values.shape[1] // 2 :]], axis=1)


def head_probs(rotated, keys, allowed):
    scores = jnp.where(allowed > 0.5, matmul_nt(rotated, keys), masked_score)
    weights = jnp.exp(scores - jnp.max(scores, axis=-1, keepdims=True))
    return weights / jnp.sum(weights, axis=-1, keepdims=True)


def ragged_split(columns, parts):
    main = columns // parts // 128 * 128
    return main, main + 128


def pre_kernel(
    z_size,
    tok_ref,
    wkv_ref,
    gains_ref,
    table_ref,
    seg_ref,
    cot_hbm,
    wq_hbm,
    wo_hbm,
    wg_hbm,
    wu_hbm,
    wd_hbm,
    n1_ref,
    rot_ref,
    key_ref,
    val_ref,
    att_ref,
    mid_ref,
    n2_ref,
    gain_ref,
    allow_ref,
    kv_out,
    wq_out,
    wo_out,
    w3_out,
    dy_out,
    kv_w,
    q_w,
    o_w,
    tok,
    part,
    part_y,
    query,
    y_send,
    y_recv,
    ky_send,
    ky_recv,
    az_send,
    az_recv,
    ax_send,
    ax_recv,
    ac_send,
    ac_recv,
    fz_send,
    fz_recv,
    fx_send,
    fx_recv,
    fc_send,
    fc_recv,
    dz_send,
    dz_recv,
    dy_send,
    dy_recv,
    local_sem,
):
    me_z, me_x = lax.axis_index("z"), lax.axis_index("x")
    me_c, me_y = lax.axis_index("c"), lax.axis_index("mp")
    own, width = tok_ref.shape
    rows = wq_hbm.shape[0]
    half_rows = wkv_ref.shape[0]
    head = key_ref.shape[1]
    main, units = ragged_split(wg_hbm.shape[1], z_size)
    to_y, to_x, to_c = {"mp": 1 - me_y}, {"x": 1 - me_x}, {"c": 1 - me_c}

    def to_z(step):
        return {"z": lax.rem(me_z + step, z_size)}

    def from_z(step):
        return lax.rem(me_z - step + z_size, z_size)

    def row_block(step, x_at, c_at):
        start = ((from_z(step) * 2 + x_at) * 2 + c_at) * rows
        return pl.ds(pl.multiple_of(start, rows), rows)

    mine = pl.ds(pl.multiple_of(me_y * own, own), own)
    theirs = pl.ds(pl.multiple_of((1 - me_y) * own, own), own)
    bufs = (kv_w, q_w, o_w)
    inputs = (None, wq_hbm, wo_hbm)

    locals_ = []

    def local(src, dst):
        copy = pltpu.make_async_copy(src, dst, local_sem.at[len(locals_)])
        copy.start()
        locals_.append(copy)
        return copy

    here = row_block(0, me_x, me_c)
    own_q = local(wq_hbm, q_w.at[here])
    own_o = local(wo_hbm, o_w.at[here])
    ffn_in = (wg_hbm, wu_hbm, wd_hbm)

    def body_of(target):
        return pl.ds(pl.multiple_of(target * main, 128), main), pl.ds(0, main)

    def tail_of(target):
        start = z_size * main + lax.rem(target + 1, 2) * 128
        return pl.ds(pl.multiple_of(start, 128), 128), pl.ds(main, 128)

    def is_inner(at):
        return (at > 0) & (at < z_size - 1)

    own_f = []
    for kind in range(3):
        src, dst = body_of(me_z)
        own_f.append(local(ffn_in[kind].at[:, src], w3_out.at[kind, here, dst]))

    def own_tail(kind):
        src, dst = tail_of(me_z)
        return pltpu.make_async_copy(
            ffn_in[kind].at[:, src], w3_out.at[kind, here, dst], local_sem.at[12 + kind]
        )

    @pl.when(is_inner(me_z))
    def _():
        for kind in range(3):
            own_tail(kind).start()
    own_d = local(cot_hbm, dy_out.at[0, mine])

    kv_own = pl.ds(pl.multiple_of(here.start + me_y * half_rows, half_rows), half_rows)
    spread = jnp.concatenate([gains_ref[...], jnp.zeros((120, 128), jnp.float32)], axis=0).T
    kv_w[kv_own, : 2 * head] = wkv_ref[...]
    kv_w[kv_own, 2 * head :] = spread[:half_rows, :].astype(jnp.bfloat16)

    barrier = pltpu.get_barrier_semaphore()
    peers = [to_y, to_x, to_c] + [to_z(step) for step in range(1, z_size)]
    for where in peers:
        pl.semaphore_signal(barrier, inc=1, device_id=where, device_id_type=MESH_ID)
    pl.semaphore_wait(barrier, len(peers))

    tok_y = remote(tok_ref, tok.at[mine], y_send.at[1], y_recv.at[1], to_y)
    tok_y_in = remote(tok_ref, tok.at[theirs], y_send.at[1], y_recv.at[1], to_y)
    part_out = remote(part.at[theirs], part_y, y_send.at[2], y_recv.at[2], to_y)
    n2_y = remote(n2_ref.at[mine], n2_ref.at[mine], y_send.at[3], y_recv.at[3], to_y)
    n2_y_in = remote(n2_ref.at[theirs], n2_ref.at[theirs], y_send.at[3], y_recv.at[3], to_y)

    def block_of(kind, step, x_at):
        if kind:
            return row_block(step, x_at, me_c)
        return kv_rows(step, x_at, me_y)

    def kv_rows(step, x_at, y_at):
        start = row_block(step, x_at, me_c).start + y_at * half_rows
        return pl.ds(pl.multiple_of(start, half_rows), half_rows)

    def kv_y(step, far):
        x_at = 1 - me_x if far else me_x
        block = kv_w.at[kv_rows(step, x_at, me_y)]
        slot = step + z_size * far
        return remote(block, block, ky_send.at[slot], ky_recv.at[slot], to_y)

    def kv_y_in(step, far):
        x_at = 1 - me_x if far else me_x
        block = kv_w.at[kv_rows(step, x_at, 1 - me_y)]
        slot = step + z_size * far
        return remote(block, block, ky_send.at[slot], ky_recv.at[slot], to_y)

    def source(kind, step):
        if isinstance(step, int) and step == 0 and kind:
            return inputs[kind]
        return bufs[kind].at[block_of(kind, step, me_x)]

    first_z, last_z = (z_size - 1 - me_z) // (z_size - 1), me_z // (z_size - 1)
    inner = first_z + last_z == 0
    order = (0, 1 + 2 * first_z, 3 - first_z - last_z, 2 - first_z + last_z)
    hops = (
        None,
        (lax.rem(me_z + 1, z_size), 2),
        (lax.rem(me_z + z_size - 1, z_size), 2),
        (lax.rem(3 * (me_z + 3), z_size), lax.rem(2 * me_z + 3, z_size)),
    )

    def a_z_own(kind, right):
        return remote(
            source(kind, 0),
            bufs[kind].at[block_of(kind, 0, me_x)],
            az_send.at[kind, right],
            az_recv.at[kind, 1 if right else z_size - 1],
            to_z(1 if right else z_size - 1),
        )

    def a_z_start(kind):
        @pl.when(last_z == 0)
        def _():
            a_z_own(kind, 1).start()

        @pl.when(first_z == 0)
        def _():
            a_z_own(kind, 0).start()

    def a_z(kind, index):
        target, slot = hops[index]
        block = bufs[kind].at[block_of(kind, order[index], me_x)]
        return remote(
            block, block, az_send.at[kind, 1 + index], az_recv.at[kind, slot], {"z": target}
        )

    def a_z_next(kind, index):
        @pl.when(inner)
        def _():
            a_z(kind, index).start()

    def a_z_done(kind):
        @pl.when(last_z == 0)
        def _():
            a_z_own(kind, 1).wait_send()

        @pl.when(first_z == 0)
        def _():
            a_z_own(kind, 0).wait_send()

        @pl.when(inner)
        def _():
            for index in range(1, z_size):
                a_z(kind, index).wait_send()

    def a_z_in(kind, step):
        block = bufs[kind].at[block_of(kind, step, me_x)]
        return remote(block, block, az_send.at[kind, 0], az_recv.at[kind, step], to_z(1))

    def a_x(kind, step):
        return remote(
            source(kind, step),
            bufs[kind].at[block_of(kind, step, me_x)],
            ax_send.at[kind, step],
            ax_recv.at[kind, step],
            to_x,
        )

    def a_x_in(kind, step):
        block = bufs[kind].at[block_of(kind, step, 1 - me_x)]
        return remote(block, block, ax_send.at[kind, step], ax_recv.at[kind, step], to_x)

    def a_c(kind, step, far):
        x_at = 1 - me_x if far else me_x
        block = bufs[kind].at[row_block(step, x_at, me_c)]
        src = source(kind, step) if kind and not far else block
        slot = step + z_size * far
        return remote(src, block, ac_send.at[kind, slot], ac_recv.at[kind, slot], to_c)

    def a_c_in(kind, step, far):
        x_at = 1 - me_x if far else me_x
        block = bufs[kind].at[row_block(step, x_at, 1 - me_c)]
        slot = step + z_size * far
        return remote(block, block, ac_send.at[kind, slot], ac_recv.at[kind, slot], to_c)

    def f_z(kind, step, act):
        target = lax.rem(me_z + step, z_size)

        def piece(index, src, dst):
            return remote(
                ffn_in[kind].at[:, src],
                w3_out.at[kind, here, dst],
                fz_send.at[kind, step, index],
                fz_recv.at[kind, step, index],
                to_z(step),
            )

        act(piece(0, *body_of(target)))

        @pl.when(is_inner(target))
        def _():
            act(piece(1, *tail_of(target)))

    def f_z_wait(kind, step):
        block = row_block(step, me_x, me_c)

        def piece(index, dst):
            part = w3_out.at[kind, block, dst]
            return remote(
                part, part, fz_send.at[kind, step, index], fz_recv.at[kind, step, index], to_z(step)
            )

        piece(0, pl.ds(0, main)).wait_recv()

        @pl.when(inner)
        def _():
            piece(1, pl.ds(main, 128)).wait_recv()

    def f_x(kind, step, x_at, act):
        for case, columns in ((inner, units), (first_z + last_z > 0, main)):

            @pl.when(case)
            def _(columns=columns):
                block = w3_out.at[kind, row_block(step, x_at, me_c), pl.ds(0, columns)]
                act(remote(block, block, fx_send.at[kind, step], fx_recv.at[kind, step], to_x))

    def f_x_start(kind, step):
        f_x(kind, step, me_x, lambda copy: copy.start())

    def f_x_wait(kind, step):
        f_x(kind, step, 1 - me_x, lambda copy: copy.wait_recv())

    def f_x_done(kind, step):
        f_x(kind, step, me_x, lambda copy: copy.wait_send())

    def f_c(kind, step, far):
        block = w3_out.at[kind, row_block(step, 1 - me_x if far else me_x, me_c)]
        slot = step + z_size * far
        return remote(block, block, fc_send.at[kind, slot], fc_recv.at[kind, slot], to_c)

    def f_c_in(kind, step, far):
        block = w3_out.at[kind, row_block(step, 1 - me_x if far else me_x, 1 - me_c)]
        slot = step + z_size * far
        return remote(block, block, fc_send.at[kind, slot], fc_recv.at[kind, slot], to_c)

    def d_source(step):
        return cot_hbm if isinstance(step, int) else dy_out.at[step, mine]

    def d_z_own(right):
        slot = 1 if right else z_size - 1
        return remote(
            cot_hbm, dy_out.at[slot, mine], dz_send.at[right], dz_recv.at[slot], to_z(slot)
        )

    def d_z_start():
        @pl.when(last_z == 0)
        def _():
            d_z_own(1).start()

        @pl.when(first_z == 0)
        def _():
            d_z_own(0).start()

    def d_z(index):
        target, slot = hops[index]
        return remote(
            dy_out.at[order[index], mine],
            dy_out.at[slot, mine],
            dz_send.at[1 + index],
            dz_recv.at[slot],
            {"z": target},
        )

    def d_z_done():
        @pl.when(last_z == 0)
        def _():
            d_z_own(1).wait_send()

        @pl.when(first_z == 0)
        def _():
            d_z_own(0).wait_send()

        @pl.when(inner)
        def _():
            for index in range(1, z_size):
                d_z(index).wait_send()

    def d_z_in(step):
        block = dy_out.at[step, mine]
        return remote(block, block, dz_send.at[0], dz_recv.at[step], to_z(1))

    def d_y(step):
        return remote(
            d_source(step), dy_out.at[step, mine], dy_send.at[step], dy_recv.at[step], to_y
        )

    def d_y_in(step):
        block = dy_out.at[step, theirs]
        return remote(block, block, dy_send.at[step], dy_recv.at[step], to_y)

    for kind in (1, 0, 2):
        a_z_start(kind)
        a_x(kind, 0).start()
    kv_y(0, 0).start()
    tok_y.start()
    for kind in (1, 2):
        a_c(kind, 0, 0).start()
    tok[mine, :] = tok_ref[...]
    seq = 2 * own
    query_at = lax.broadcasted_iota(jnp.int32, (seq, seq), 0)
    key_at = lax.broadcasted_iota(jnp.int32, (seq, seq), 1)
    same = seg_ref[...].T[:, :1] == seg_ref[:1, :]
    allowed = same & (key_at <= query_at) & (query_at - key_at < WINDOW)
    allow_ref[...] = jnp.where(allowed, 1.0, 0.0)
    d_y(0).start()

    def from_x(index):
        step = order[index]
        for kind in (1, 0, 2):
            a_x_in(kind, step).wait_recv()
            if kind:
                a_c(kind, step, 1).start()
            else:
                kv_y(step, 1).start()

    def from_y(index):
        step = order[index]
        for far in range(2):
            kv_y_in(step, far).wait_recv()
            a_c(0, step, far).start()

    for index in range(1, z_size):
        step = order[index]
        for kind in (1, 0, 2):
            a_z_in(kind, step).wait_recv()
            a_z_next(kind, index)
            a_x(kind, step).start()
            if kind:
                a_c(kind, step, 0).start()
            else:
                kv_y(step, 0).start()
        if index == z_size - 2:
            d_z_start()
        if index == z_size - 1:
            for copy in own_f:
                copy.wait()

            @pl.when(inner)
            def _():
                for kind in range(3):
                    own_tail(kind).wait()

            for kind in range(3):
                for away in (1, 3, 2):
                    f_z(kind, away, lambda copy: copy.start())
            for kind in range(3):
                f_x_start(kind, 0)
                f_c(kind, 0, 0).start()
        if index >= 2:
            from_x(index - 2)
            from_y(index - 2)
    for index in (z_size - 2, z_size - 1):
        from_x(index)
        from_y(index)

    def hand_on(kind, step):
        f_z_wait(kind, step)
        f_x_start(kind, step)
        f_c(kind, step, 0).start()

    def cross(kind, step):
        f_x_wait(kind, step)
        f_c(kind, step, 1).start()

    def pass_cotangent(step):
        d_z_in(order[step]).wait_recv()

        @pl.when(inner)
        def _():
            d_z(step).start()

        d_y(order[step]).start()

    tok_y_in.wait_recv()
    own_q.wait()
    own_o.wait()
    for kind in (0, 1):
        for step in range(z_size):
            for far in range(2):
                a_c_in(kind, step, far).wait_recv()

    gains = kv_w[:, 2 * head :].astype(jnp.float32).T[:8, :]
    gain_ref[...] = gains

    def norm_rows(index, carry):
        at = pl.ds(pl.multiple_of(index * 32, 32), 32)
        values = tok[at, :].astype(jnp.float32)
        scale = lax.rsqrt(jnp.mean(values * values, axis=-1, keepdims=True) + epsilon)
        n1_ref[at, :] = (values * scale * gain_ref[0:1, :]).astype(jnp.bfloat16)
        return carry

    lax.fori_loop(0, 2 * own // 32, norm_rows, 0)
    hand_on(0, 1)
    table = (table_ref[0], table_ref[1])
    key_ref[...] = spin(dot_nn(n1_ref[...], kv_w[:, :head]), table).astype(jnp.bfloat16)
    val_ref[...] = dot_nn(n1_ref[...], kv_w[:, head : 2 * head]).astype(jnp.bfloat16)
    hand_on(0, 3)
    head_scale = head ** (-0.5)
    heads = att_ref.shape[1] // head

    half_cols = att_ref.shape[1] // 2
    for index in range(2):
        cols = pl.ds(index * half_cols, half_cols)
        query[:, cols] = dot_nn(n1_ref[...], q_w[:, cols])

    def attend(index):
        cols = pl.ds(index * head, head)
        rotated = (spin(query[:, cols], table) * head_scale).astype(jnp.bfloat16)
        rot_ref[:, cols] = rotated
        probs = head_probs(rotated, key_ref[...], allow_ref[...]).astype(jnp.bfloat16)
        att_ref[:, cols] = dot_nn(probs, val_ref[...]).astype(jnp.bfloat16)

    tasks = [
        lambda: hand_on(0, 2),
        lambda: pass_cotangent(1),
        lambda: hand_on(1, 1),
        lambda: cross(0, 0),
        lambda: hand_on(1, 3),
    ]
    for index in range(heads):
        attend(index)
        if index < len(tasks):
            tasks[index]()
    for step in range(z_size):
        for far in range(2):
            a_c_in(2, step, far).wait_recv()
    saves = [
        local(kv_w, kv_out),
        local(q_w, wq_out),
        local(o_w, wo_out),
    ]
    span = width // 4

    def project(index, carry):
        cols = pl.ds(pl.multiple_of(index * span, span), span)
        part[:, cols] = matmul_nt(att_ref[...], o_w[cols, :]).astype(jnp.bfloat16)
        return carry

    lax.fori_loop(0, 4, project, 0)
    part_out.start()
    hand_on(1, 2)
    cross(1, 0)
    cross(2, 0)
    cross(0, 1)
    pass_cotangent(2)
    hand_on(2, 1)
    part_out.wait_recv()

    def middle(index, carry):
        at = pl.ds(pl.multiple_of(index * 32, 32), 32)
        there = pl.ds(pl.multiple_of(me_y * own + index * 32, 32), 32)
        values = (
            tok_ref[at, :].astype(jnp.float32)
            + part[there, :].astype(jnp.float32)
            + part_y[at, :].astype(jnp.float32)
        )
        mid_ref[at, :] = values
        scale = lax.rsqrt(jnp.mean(values * values, axis=-1, keepdims=True) + epsilon)
        n2_ref[there, :] = (values * scale * gain_ref[1:2, :]).astype(jnp.bfloat16)
        return carry

    lax.fori_loop(0, own // 32, middle, 0)
    n2_y.start()
    hand_on(2, 3)
    cross(0, 3)
    pass_cotangent(3)
    hand_on(2, 2)
    cross(0, 2)
    for kind in (1, 2):
        for step in (1, 3, 2):
            cross(kind, step)
    for kind in range(3):
        for step in range(z_size):
            for far in range(2):
                f_c_in(kind, step, far).wait_recv()
    for step in range(z_size):
        d_y_in(step).wait_recv()
    n2_y_in.wait_recv()

    for kind in range(3):
        a_z_done(kind)
    d_z_done()
    tok_y.wait_send()
    part_out.wait_send()
    n2_y.wait_send()
    own_d.wait()
    for copy in saves:
        copy.wait()
    for step in range(z_size):
        d_y(step).wait_send()
        for far in range(2):
            kv_y(step, far).wait_send()
        for kind in range(3):
            if step:
                f_z(kind, step, lambda copy: copy.wait_send())
            a_x(kind, step).wait_send()
            f_x_done(kind, step)
            for far in range(2):
                a_c(kind, step, far).wait_send()
                f_c(kind, step, far).wait_send()


def pre_call(tokens, w_kv, gains, table, segments, cotangent, w_query, w_out, ffn):
    z_size = lax.axis_size("z")
    own, width = tokens.shape
    seq = 2 * own
    rows, cols = w_query.shape
    head = table.shape[2] * 2
    units = ragged_split(ffn[0].shape[1], z_size)[1]
    low = lambda *dims: jax.ShapeDtypeStruct(dims, jnp.bfloat16)
    full = lambda *dims: jax.ShapeDtypeStruct(dims, jnp.float32)
    dma = lambda *lead: pltpu.SemaphoreType.DMA(lead)
    vmem = pl.BlockSpec(memory_space=pltpu.VMEM)
    hbm = pl.BlockSpec(memory_space=pl.ANY)
    wide = lambda *lead: pltpu.VMEM((*lead, width), jnp.bfloat16)
    return pl.pallas_call(
        functools.partial(pre_kernel, z_size),
        out_shape=(
            low(seq, width),
            low(seq, cols),
            low(seq, head),
            low(seq, head),
            low(seq, cols),
            full(own, width),
            low(seq, width),
            full(8, width),
            full(seq, seq),
            low(width, 2 * head + 128),
            low(width, cols),
            low(width, cols),
            low(3, width, units),
            low(z_size, seq, width),
        ),
        in_specs=[vmem] * 5 + [hbm] * 6,
        out_specs=(vmem,) * 9 + (hbm,) * 5,
        scratch_shapes=[
            pltpu.VMEM((width, 2 * head + 128), jnp.bfloat16),
            pltpu.VMEM((width, cols), jnp.bfloat16),
            pltpu.VMEM((width, cols), jnp.bfloat16),
            wide(seq),
            wide(seq),
            wide(own),
            pltpu.VMEM((seq, cols), jnp.float32),
            dma(4),
            dma(4),
            dma(2 * z_size),
            dma(2 * z_size),
            dma(3, z_size + 1),
            dma(3, z_size),
            dma(3, z_size),
            dma(3, z_size),
            dma(3, 2 * z_size),
            dma(3, 2 * z_size),
            dma(3, z_size, 2),
            dma(3, z_size, 2),
            dma(3, z_size),
            dma(3, z_size),
            dma(3, 2 * z_size),
            dma(3, 2 * z_size),
            dma(z_size + 1),
            dma(z_size),
            dma(z_size),
            dma(z_size),
            dma(16),
        ],
        compiler_params=pltpu.CompilerParams(
            collective_id=1, has_side_effects=True, vmem_limit_bytes=VMEM_BYTES
        ),
        cost_estimate=pl.CostEstimate(
            flops=8 * seq * width * cols,
            bytes_accessed=8 * width * (cols + units),
            transcendentals=seq * seq * cols // head,
        ),
    )(tokens, w_kv, gains, table, segments, cotangent, w_query, w_out, *ffn)


def post_kernel(
    z_size,
    main,
    tok_ref,
    gain_ref,
    gain_part_ref,
    n1_ref,
    rot_ref,
    key_ref,
    val_ref,
    att_ref,
    table_ref,
    allow_ref,
    kv_hbm,
    wq_hbm,
    wo_hbm,
    mix_hbm,
    gmf_hbm,
    gmb_hbm,
    mid_hbm,
    sums_hbm,
    mixed_ref,
    tgrad_ref,
    gsum_ref,
    kvg_ref,
    qg_ref,
    og_ref,
    ffn_out,
    kv_w,
    q_w,
    o_w,
    o_part,
    gm,
    gm_f,
    gq,
    gkv,
    kv_sum,
    back_y,
    mix_y,
    mix_z,
    mix_s,
    o_c,
    o_x,
    o_z,
    q_c,
    q_x,
    q_z,
    kv_y,
    kv_c,
    kv_x,
    kv_z,
    gain_own,
    gain_in,
    ffn_in,
    ffn_own,
    load_sem,
    own_sem,
    fx_send,
    fx_recv,
    fz_send,
    fz_recv,
    y_send,
    y_recv,
    my_send,
    my_recv,
    mz_send,
    mz_recv,
    wc_send,
    wc_recv,
    wx_send,
    wx_recv,
    wz_send,
    wz_recv,
    kc_send,
    kc_recv,
    kz_send,
    kz_recv,
    g_send,
    g_recv,
):
    me_z, me_x = lax.axis_index("z"), lax.axis_index("x")
    me_c, me_y = lax.axis_index("c"), lax.axis_index("mp")
    own, width = tok_ref.shape
    seq = 2 * own
    head = key_ref.shape[1]
    cols_here = att_ref.shape[1]
    heads = cols_here // head
    rows = qg_ref.shape[0]
    span = width // z_size
    mine = pl.ds(pl.multiple_of(me_y * own, own), own)
    theirs = pl.ds(pl.multiple_of((1 - me_y) * own, own), own)
    to_y, to_x, to_c = {"mp": 1 - me_y}, {"x": 1 - me_x}, {"c": 1 - me_c}
    head_scale = head ** (-0.5)

    def behind(step):
        return lax.rem(me_z - step + z_size, z_size)

    def to_z(step):
        return {"z": lax.rem(me_z + step, z_size)}

    def row_block(step, x_at, c_at):
        start = ((behind(step) * 2 + x_at) * 2 + c_at) * rows
        return pl.ds(pl.multiple_of(start, rows), rows)

    loads = [
        pltpu.make_async_copy(wo_hbm, o_w, load_sem.at[0]),
        pltpu.make_async_copy(wq_hbm, q_w, load_sem.at[1]),
        pltpu.make_async_copy(
            kv_hbm.at[:, :, :, :, :, pl.ds(0, 2 * head)], kv_w, load_sem.at[2]
        ),
    ]
    for step in range(z_size):
        loads.append(
            pltpu.make_async_copy(mix_hbm.at[step, me_y], mix_s.at[step], load_sem.at[3 + step])
        )
    loads.append(pltpu.make_async_copy(gmf_hbm, gm_f, load_sem.at[3 + z_size]))
    loads.append(pltpu.make_async_copy(gmb_hbm, gm.at[mine], load_sem.at[4 + z_size]))
    mid_load = pltpu.make_async_copy(mid_hbm, gm_f, load_sem.at[5 + z_size])
    for load in loads:
        load.start()

    barrier = pltpu.get_barrier_semaphore()
    peers = [to_y, to_x, to_c] + [to_z(step) for step in range(1, z_size)]
    for where in peers:
        pl.semaphore_signal(barrier, inc=1, device_id=where, device_id_type=MESH_ID)
    pl.semaphore_wait(barrier, len(peers))

    tasks = [(step, kind) for step in (2, 3) for kind in range(3)]

    def f_x(index):
        step, kind = tasks[index]
        return remote(
            sums_hbm.at[kind, step, 1],
            ffn_in.at[index],
            fx_send.at[index],
            fx_recv.at[index],
            to_x,
        )

    def f_own(index):
        step, kind = tasks[index]
        return pltpu.make_async_copy(
            sums_hbm.at[kind, step, 0], ffn_own.at[index % 2], own_sem.at[index % 2]
        )

    def f_z(step, kind, source_z, act):
        for case, columns in (
            ((source_z > 0) & (source_z < z_size - 1), ffn_out.shape[3]),
            ((source_z == 0) | (source_z == z_size - 1), main),
        ):

            @pl.when(case)
            def _(columns=columns):
                cols = pl.ds(0, columns)
                if step == 1:
                    src = sums_hbm.at[kind, 1, 0, :, cols]
                else:
                    src = ffn_in.at[tasks.index((step, kind)), :, cols]
                act(
                    remote(
                        src,
                        ffn_out.at[kind, step, :, cols],
                        fz_send.at[kind, step],
                        fz_recv.at[kind, step],
                        to_z(step),
                    )
                )

    def tick(index):
        step, kind = tasks[index]
        f_x(index).wait_recv()
        f_own(index).wait()
        block = ffn_in.at[index]
        add_rows(block, [ffn_own.at[index % 2]], block, rows)
        if index + 2 < len(tasks):
            f_own(index + 2).start()
        f_z(step, kind, me_z, lambda copy: copy.start())

    def f_x_own(kind):
        return remote(
            sums_hbm.at[kind, 0, 1],
            ffn_out.at[kind, 0],
            fx_send.at[len(tasks) + kind],
            fx_recv.at[len(tasks) + kind],
            to_x,
        )

    f_own(0).start()
    f_own(1).start()
    for index in range(len(tasks)):
        f_x(index).start()
    for kind in range(3):
        f_z(1, kind, me_z, lambda copy: copy.start())

    gm_y = remote(gmb_hbm, gm.at[mine], y_send.at[0], y_recv.at[0], to_y)
    gm_y_in = remote(gm.at[theirs], gm.at[theirs], y_send.at[0], y_recv.at[0], to_y)
    gm_y.start()

    first_z, last_z = (z_size - 1 - me_z) // (z_size - 1), me_z // (z_size - 1)
    inner = first_z + last_z == 0
    order = (
        0,
        1 + (me_z + 1) // 2,
        2 + (2 * me_z - 3) * (1 - first_z - last_z),
        3 - 2 * (me_z // 2),
    )
    right = (None, 1 - me_z // 2, (3 - me_z) * (2 - me_z) // 6 + me_z // 2 * (1 - last_z), 1 - me_z // 2)

    def hop_slot(index):
        step, way = order[index], right[index]
        return way * lax.rem(step + 1, z_size) + (1 - way) * (step - 1 + 4 * ((3 - step) // 2))

    def hop_target(index):
        return {"z": me_z + 2 * right[index] - 1}

    def mix_over_y(step):
        return remote(
            mix_hbm.at[step, 1 - me_y], mix_y.at[step], my_send.at[step], my_recv.at[step], to_y
        )

    def mix_over_z(index):
        slot = hop_slot(index)
        return remote(
            mix_s.at[order[index]],
            mix_z.at[slot],
            mz_send.at[index],
            mz_recv.at[slot],
            hop_target(index),
        )

    def mix_z_in(slot):
        return remote(mix_z.at[slot], mix_z.at[slot], mz_send.at[1], mz_recv.at[slot], to_z(1))

    def mix_add(step, others, last):
        def add_tile(tile, carry):
            at = pl.ds(pl.multiple_of(tile * TILE, TILE), TILE)
            total = mix_s[step, at, :].astype(jnp.float32)
            for other in others:
                total = total + other[at, :].astype(jnp.float32)
            if last:
                mixed_ref[:, at] = (gm_f[:, at] + total.T).astype(jnp.bfloat16)
            else:
                mix_s[step, at, :] = total.astype(jnp.bfloat16)
            return carry

        lax.fori_loop(0, width // TILE, add_tile, 0)

    def mix_step(index):
        step = order[index]
        mix_over_y(step).wait_recv()
        from_y = mix_y.at[step]
        if index:

            @pl.when(inner)
            def _():
                mix_z_in(step).wait_recv()
                mix_add(step, [from_y, mix_z.at[step]], False)

            @pl.when(first_z + last_z > 0)
            def _():
                mix_add(step, [from_y], False)

            mix_over_z(index).start()
        else:
            mid_load.wait()

            @pl.when(first_z == 0)
            def _():
                mix_z_in(0).wait_recv()

            @pl.when(last_z == 0)
            def _():
                mix_z_in(z_size).wait_recv()

            @pl.when(inner)
            def _():
                mix_add(0, [from_y, mix_z.at[0], mix_z.at[z_size]], True)

            @pl.when(first_z > 0)
            def _():
                mix_add(0, [from_y, mix_z.at[z_size]], True)

            @pl.when(last_z > 0)
            def _():
                mix_add(0, [from_y, mix_z.at[0]], True)

    for index in (1, 2, 3, 0):
        mix_over_y(order[index]).start()

    kinds = ((o_part, o_c, o_x, o_z, og_ref), (o_w, q_c, q_x, q_z, qg_ref))

    def w_c(kind, step, far):
        x_at = 1 - me_x if far else me_x
        return remote(
            kinds[kind][0].at[row_block(step, x_at, 1 - me_c)],
            kinds[kind][1].at[step, far],
            wc_send.at[kind, step, far],
            wc_recv.at[kind, step, far],
            to_c,
        )

    def w_x(kind, step):
        return remote(
            kinds[kind][0].at[row_block(step, 1 - me_x, me_c)],
            kinds[kind][2].at[step],
            wx_send.at[kind, step],
            wx_recv.at[kind, step],
            to_x,
        )

    def w_z(kind, index):
        step, slot = order[index], hop_slot(index)
        return remote(
            kinds[kind][0].at[row_block(step, me_x, me_c)],
            kinds[kind][3].at[slot],
            wz_send.at[kind, index],
            wz_recv.at[kind, slot],
            hop_target(index),
        )

    def w_z_in(kind, slot):
        block = kinds[kind][3].at[slot]
        return remote(block, block, wz_send.at[kind, 1], wz_recv.at[kind, slot], to_z(1))

    def w_x_stage(kind, index):
        step = order[index]
        w_c(kind, step, 1).wait_recv()
        block = kinds[kind][0].at[row_block(step, 1 - me_x, me_c)]
        add_rows(block, [kinds[kind][1].at[step, 1]], block, rows)
        w_x(kind, step).start()

    def w_z_stage(kind, index):
        part, from_c, from_x, from_z, result = kinds[kind]
        step = order[index]
        w_c(kind, step, 0).wait_recv()
        w_x(kind, step).wait_recv()
        block = part.at[row_block(step, me_x, me_c)]
        others = [from_c.at[step, 0], from_x.at[step]]
        if index:

            @pl.when(inner)
            def _():
                w_z_in(kind, step).wait_recv()
                add_rows(block, [*others, from_z.at[step]], block, rows)

            @pl.when(first_z + last_z > 0)
            def _():
                add_rows(block, others, block, rows)

            w_z(kind, index).start()
        else:

            @pl.when(first_z == 0)
            def _():
                w_z_in(kind, 0).wait_recv()

            @pl.when(last_z == 0)
            def _():
                w_z_in(kind, z_size).wait_recv()

            @pl.when(inner)
            def _():
                add_rows(block, [*others, from_z.at[0], from_z.at[z_size]], result, rows)

            @pl.when(first_z > 0)
            def _():
                add_rows(block, [*others, from_z.at[z_size]], result, rows)

            @pl.when(last_z > 0)
            def _():
                add_rows(block, [*others, from_z.at[0]], result, rows)

    def w_product(kind, index, left, values):
        step = order[index]
        at = pl.ds(pl.multiple_of(behind(step) * span, 128), span)
        turned = left[:, at].T

        def tile_body(tile, carry):
            cols = pl.ds(pl.multiple_of(tile * TILE, TILE), TILE)
            kinds[kind][0][at, cols] = dot_nn(turned, values[:, cols]).astype(jnp.bfloat16)
            return carry

        lax.fori_loop(0, cols_here // TILE, tile_body, 0)
        for far in (1, 0):
            w_c(kind, step, far).start()

    tick(0)
    tick(1)
    loads[-1].wait()
    gm_y_in.wait_recv()
    w_product(0, 1, gm, att_ref)
    w_product(0, 2, gm, att_ref)
    w_x_stage(0, 1)
    w_product(0, 3, gm, att_ref)
    w_x_stage(0, 2)
    tick(2)
    w_product(0, 0, gm, att_ref)
    w_x_stage(0, 3)
    for load in loads[:-1]:
        load.wait()

    kv_sum[...] = jnp.zeros(kv_sum.shape, jnp.float32)
    table = (table_ref[0], table_ref[1])

    for index in range(2):
        cols = pl.ds(index * (cols_here // 2), cols_here // 2)
        gq[:, cols] = dot_nn(gm[...], o_w[:, cols]).astype(jnp.bfloat16)

    def attend_back(index):
        cols = pl.ds(index * head, head)
        grad_vals = gq[:, cols]
        rotated = rot_ref[:, cols]
        probs = head_probs(rotated, key_ref[...], allow_ref[...])
        grad_probs = matmul_nt(grad_vals, val_ref[...])
        delta = jnp.sum(probs * grad_probs, axis=-1, keepdims=True)
        grad_scores = (probs * (grad_probs - delta)).astype(jnp.bfloat16)
        grad_rot = dot_nn(grad_scores, key_ref[...])
        gq[:, cols] = (spin_back(grad_rot, table) * head_scale).astype(jnp.bfloat16)
        kv_sum[0] += matmul_tn(grad_scores, rotated)
        kv_sum[1] += matmul_tn(probs.astype(jnp.bfloat16), grad_vals)

    for index in range(heads):
        attend_back(index)
        if index == 0:
            w_x_stage(0, 0)
        if 3 + index < len(tasks):
            tick(3 + index)
        if index == heads - 1:
            mix_step(1)
    gkv[:, :head] = spin_back(kv_sum[0], table).astype(jnp.bfloat16)
    gkv[:, head:] = kv_sum[1].astype(jnp.bfloat16)

    w_product(1, 1, n1_ref, gq)
    w_product(1, 2, n1_ref, gq)
    w_x_stage(1, 1)
    w_z_stage(0, 1)
    w_product(1, 3, n1_ref, gq)
    w_x_stage(1, 2)
    w_product(1, 0, n1_ref, gq)
    w_x_stage(1, 3)
    w_x_stage(1, 0)
    for kind in range(3):
        f_x_own(kind).start()

    gm_y.wait_send()
    back = gm
    def input_tile(index, carry):
        at = pl.ds(pl.multiple_of(index * span, 128), span)
        back[:, at] = (
            matmul_nt(gq[...], q_w[at, :]) + matmul_nt(gkv[...], kv_w[index].reshape(span, 2 * head))
        ).astype(jnp.bfloat16)
        return carry

    lax.fori_loop(0, z_size, input_tile, 0)
    back_out = remote(back.at[theirs], back_y, y_send.at[1], y_recv.at[1], to_y)
    back_out.start()

    kv_part = kv_w

    def kv_tile(index, carry):
        at = pl.ds(pl.multiple_of(index * span, 128), span)
        product = dot_nn(n1_ref[:, at].T, gkv[...]).astype(jnp.bfloat16)
        kv_part[index] = product.reshape(kv_part.shape[1:])
        return carry

    lax.fori_loop(0, z_size, kv_tile, 0)
    kv_over_y = remote(kv_part.at[:, :, :, 1 - me_y], kv_y, y_send.at[2], y_recv.at[2], to_y)
    kv_over_y.start()
    mix_step(2)
    w_z_stage(0, 2)
    mix_step(3)
    w_z_stage(0, 3)

    back_out.wait_recv()

    def input_rows(index, total):
        at = pl.ds(pl.multiple_of(index * 32, 32), 32)
        there = pl.ds(pl.multiple_of(me_y * own + index * 32, 32), 32)
        upstream = back[there, :].astype(jnp.float32) + back_y[at, :].astype(jnp.float32)
        grad, gain_part = norm_back(
            tok_ref[at, :].astype(jnp.float32), gain_ref[0:1, :], upstream
        )
        tgrad_ref[at, :] = (gm_f[at, :] + grad).astype(jnp.bfloat16)
        return total + gain_part

    attn_gain_part = lax.fori_loop(
        0, own // 32, input_rows, jnp.zeros((1, width), jnp.float32)
    )
    for index in range(4):
        at = slice(index * span, (index + 1) * span)
        gain_own[0, index : index + 1, :] = attn_gain_part[:, at]
        gain_own[0, 4 + index : 5 + index, :] = gain_part_ref[4 + index : 5 + index, :]

    def gain_send(stage, where):
        return remote(
            gain_own.at[stage], gain_in.at[stage], g_send.at[stage], g_recv.at[stage], where
        )

    gain_hops = [gain_send(0, to_y), gain_send(1, to_c), gain_send(2, to_x)]
    gain_last = [
        remote(
            gain_own.at[3], gain_in.at[2 + step], g_send.at[2 + step], g_recv.at[2 + step], to_z(step)
        )
        for step in range(1, z_size)
    ]

    def gain_fold(stage):
        gain_hops[stage].wait_recv()
        gain_own[stage + 1] = gain_own[stage] + gain_in[stage]

    gain_hops[0].start()
    mid_load.start()
    w_z_stage(1, 1)
    w_z_stage(0, 0)
    w_z_stage(1, 2)
    gain_fold(0)
    gain_hops[1].start()
    mix_step(0)
    w_z_stage(1, 3)
    gain_fold(1)
    gain_hops[2].start()
    kv_over_y.wait_recv()

    def kv_add_y(index, carry):
        for x_at in range(2):
            for c_at in range(2):
                block = kv_part.at[index, x_at, c_at, me_y]
                block[...] = (
                    block[...].astype(jnp.float32) + kv_y[index, x_at, c_at].astype(jnp.float32)
                ).astype(jnp.bfloat16)
        return carry

    lax.fori_loop(0, z_size, kv_add_y, 0)
    kv_over_c = remote(
        kv_part.at[:, :, 1 - me_c, me_y], kv_c, kc_send.at[0], kc_recv.at[0], to_c
    )
    kv_over_c.start()
    gain_fold(2)
    for copy in gain_last:
        copy.start()
    kv_over_c.wait_recv()

    def kv_add_c(index, carry):
        for x_at in range(2):
            block = kv_part.at[index, x_at, me_c, me_y]
            block[...] = (
                block[...].astype(jnp.float32) + kv_c[index, x_at].astype(jnp.float32)
            ).astype(jnp.bfloat16)
        return carry

    lax.fori_loop(0, z_size, kv_add_c, 0)
    kv_over_x = remote(
        kv_part.at[:, 1 - me_x, me_c, me_y], kv_x, kc_send.at[1], kc_recv.at[1], to_x
    )
    kv_over_x.start()
    w_z_stage(1, 0)
    kv_over_x.wait_recv()

    def kv_add_x(index, carry):
        block = kv_part.at[index, me_x, me_c, me_y]
        block[...] = (
            block[...].astype(jnp.float32) + kv_x[index].astype(jnp.float32)
        ).astype(jnp.bfloat16)
        return carry

    lax.fori_loop(0, z_size, kv_add_x, 0)
    kv_over_z = [
        remote(
            kv_part.at[lax.rem(me_z + step, z_size), me_x, me_c, me_y],
            kv_z.at[step - 1],
            kz_send.at[step],
            kz_recv.at[step],
            to_z(step),
        )
        for step in range(1, z_size)
    ]
    for copy in kv_over_z:
        copy.start()
    for copy in gain_last:
        copy.wait_recv()
    gsum_ref[...] = gain_own[3] + gain_in[3] + gain_in[4] + gain_in[5]
    for copy in kv_over_z:
        copy.wait_recv()
    kvg_ref[...] = (
        kv_part[me_z, me_x, me_c, me_y].astype(jnp.float32)
        + kv_z[0].astype(jnp.float32)
        + kv_z[1].astype(jnp.float32)
        + kv_z[2].astype(jnp.float32)
    )

    back_out.wait_send()
    kv_over_y.wait_send()
    kv_over_c.wait_send()
    kv_over_x.wait_send()
    for kind in range(3):
        f_x_own(kind).wait()
    for index in range(len(tasks)):
        f_x(index).wait_send()
    for step in range(1, z_size):
        for kind in range(3):
            f_z(step, kind, me_z, lambda copy: copy.wait_send())
            f_z(step, kind, behind(step), lambda copy: copy.wait_recv())
    for copy in gain_hops + gain_last + kv_over_z:
        copy.wait_send()
    for step in range(z_size):
        mix_over_y(step).wait_send()
        if step:
            mix_over_z(step).wait_send()
        for kind in range(2):
            w_c(kind, step, 0).wait_send()
            w_c(kind, step, 1).wait_send()
            w_x(kind, step).wait_send()
            if step:
                w_z(kind, step).wait_send()


def post_call(
    tokens,
    gains,
    gain_part,
    normed_one,
    rotated,
    keys,
    values,
    attn_vals,
    table,
    allowed,
    kv_weight,
    query_weight,
    out_weight,
    mix_parts,
    grad_mid,
    grad_mid_low,
    mid,
    ffn_sums,
    main,
):
    z_size = lax.axis_size("z")
    own, width = tokens.shape
    seq = 2 * own
    head = keys.shape[1]
    cols = attn_vals.shape[1]
    rows = width // (4 * z_size)
    units = ffn_sums.shape[4]
    low = lambda *dims: pltpu.VMEM(dims, jnp.bfloat16)
    full = lambda *dims: pltpu.VMEM(dims, jnp.float32)
    out_full = lambda *dims: jax.ShapeDtypeStruct(dims, jnp.float32)
    out_low = lambda *dims: jax.ShapeDtypeStruct(dims, jnp.bfloat16)
    dma = lambda *lead: pltpu.SemaphoreType.DMA(lead)
    vmem = pl.BlockSpec(memory_space=pltpu.VMEM)
    hbm = pl.BlockSpec(memory_space=pl.ANY)
    z = z_size
    return pl.pallas_call(
        functools.partial(post_kernel, z_size, main),
        out_shape=(
            out_low(own, width),
            out_low(own, width),
            out_full(8, width // z),
            out_full(rows // 2, 2 * head),
            out_full(rows, cols),
            out_full(rows, cols),
            out_low(3, z, rows, units),
        ),
        in_specs=[vmem] * 10 + [hbm] * 8,
        out_specs=(vmem,) * 6 + (hbm,),
        scratch_shapes=[
            low(z, 2, 2, 2, rows // 2, 2 * head),
            low(width, cols),
            low(width, cols),
            low(width, cols),
            low(seq, width),
            full(own, width),
            low(seq, cols),
            low(seq, 2 * head),
            full(2, seq, head),
            low(own, width),
            low(z, width, own),
            low(z + 1, width, own),
            low(z, width, own),
            low(z, 2, rows, cols),
            low(z, rows, cols),
            low(z + 1, rows, cols),
            low(z, 2, rows, cols),
            low(z, rows, cols),
            low(z + 1, rows, cols),
            low(z, 2, 2, rows // 2, 2 * head),
            low(z, 2, rows // 2, 2 * head),
            low(z, rows // 2, 2 * head),
            low(z - 1, rows // 2, 2 * head),
            full(4, 8, width // z),
            full(6, 8, width // z),
            low(6, rows, units),
            low(2, rows, units),
            dma(6 + z),
            dma(2),
            dma(9),
            dma(9),
            dma(3, z),
            dma(3, z),
            dma(3),
            dma(3),
            dma(z),
            dma(z),
            dma(z),
            dma(z + 1),
            dma(2, z, 2),
            dma(2, z, 2),
            dma(2, z),
            dma(2, z),
            dma(2, z),
            dma(2, z + 1),
            dma(2),
            dma(2),
            dma(z),
            dma(z),
            dma(6),
            dma(6),
        ],
        compiler_params=pltpu.CompilerParams(
            collective_id=2, has_side_effects=True, vmem_limit_bytes=VMEM_BYTES
        ),
        cost_estimate=pl.CostEstimate(
            flops=14 * seq * width * cols,
            bytes_accessed=10 * width * cols,
            transcendentals=seq * seq * cols // head,
        ),
    )(
        tokens,
        gains,
        gain_part,
        normed_one,
        rotated,
        keys,
        values,
        attn_vals,
        table,
        allowed,
        kv_weight.reshape(z, 2, 2, 2, rows // 2, kv_weight.shape[1]),
        query_weight,
        out_weight,
        mix_parts,
        grad_mid,
        grad_mid_low,
        mid,
        ffn_sums,
    )


def layout_kernel(
    z_size,
    main,
    sum_ref,
    ffn_ref,
    q_ref,
    o_ref,
    kv_ref,
    mixed_in,
    tgrad_in,
    wg_ref,
    wu_ref,
    wd_ref,
    qg_ref,
    og_ref,
    kvg_ref,
    mixed_ref,
    tgrad_ref,
):
    me_z = lax.axis_index("z")
    for kind, out in enumerate((wg_ref, wu_ref, wd_ref)):
        for step in range(z_size):
            at = lax.rem(me_z - step + z_size, z_size)
            values = ffn_ref[kind, step].astype(jnp.float32)
            if step == 0:
                values = values + sum_ref[kind, 0, 0].astype(jnp.float32)
            body = pl.ds(pl.multiple_of(at * main, 128), main)
            out[:, body] = values[:, :main]

            @pl.when((at > 0) & (at < z_size - 1))
            def _(out=out, at=at, values=values):
                tail = z_size * main + lax.rem(at + 1, 2) * 128
                out[:, pl.ds(pl.multiple_of(tail, 128), 128)] = values[:, main:]
    qg_ref[...] = q_ref[...]
    og_ref[...] = o_ref[...]
    kvg_ref[...] = kv_ref[...]
    mixed_ref[...] = mixed_in[...]
    tgrad_ref[...] = tgrad_in[...]


def layout_call(ffn_sums, ffn_grads, query_grad, out_grad, kv_grad, mixed, tokens_grad, ffn_cols):
    z_size = lax.axis_size("z")
    main, units = ragged_split(ffn_cols, z_size)
    rows, cols = query_grad.shape
    parts = rows // 16
    kv_rows = kv_grad.shape[0] // parts
    full = lambda *dims: jax.ShapeDtypeStruct(dims, jnp.float32)
    row = lambda height, width: pl.BlockSpec((height, width), lambda index: (index, 0))
    own, width = mixed.shape
    share = pl.BlockSpec((own, width // parts), lambda index: (0, index))
    specs = [row(16, cols), row(16, cols), row(kv_rows, kv_grad.shape[1]), share, share]
    return pl.pallas_call(
        functools.partial(layout_kernel, z_size, main),
        grid=(parts,),
        out_shape=(
            *[full(rows, ffn_cols)] * 3,
            full(rows, cols),
            full(rows, cols),
            full(*kv_grad.shape),
            jax.ShapeDtypeStruct(mixed.shape, jnp.bfloat16),
            jax.ShapeDtypeStruct(mixed.shape, jnp.bfloat16),
        ),
        in_specs=[
            pl.BlockSpec((3, 1, 1, 16, units), lambda index: (0, 0, 0, index, 0)),
            pl.BlockSpec((3, z_size, 16, units), lambda index: (0, 0, index, 0)),
            *specs,
        ],
        out_specs=(*[row(16, ffn_cols)] * 3, *specs),
        compiler_params=pltpu.CompilerParams(vmem_limit_bytes=VMEM_BYTES),
    )(ffn_sums, ffn_grads, query_grad, out_grad, kv_grad, mixed, tokens_grad)


FF_SPLIT = 4


def ffn_pass(normed, grad_out, gate_weight, up_weight, down_weight):
    gate = jnp.dot(normed, gate_weight, preferred_element_type=jnp.float32)
    up_proj = jnp.dot(normed, up_weight, preferred_element_type=jnp.float32)
    grad_hidden = jnp.dot(grad_out, down_weight, preferred_element_type=jnp.float32)
    product, pull = jax.vjp(gelu_product, gate, up_proj)
    hidden = product.astype(jnp.bfloat16)
    grad_gate_f, grad_up_f = pull(grad_hidden)
    grad_gate = grad_gate_f.astype(jnp.bfloat16)
    grad_up = grad_up_f.astype(jnp.bfloat16)
    mixed_part = matmul_nt(hidden, down_weight).astype(jnp.bfloat16)
    normed_part = (matmul_nt(grad_gate, gate_weight) + matmul_nt(grad_up, up_weight)).astype(
        jnp.bfloat16
    )
    weight_parts = [
        matmul_tn(normed, grad_gate).astype(jnp.bfloat16),
        matmul_tn(normed, grad_up).astype(jnp.bfloat16),
        matmul_tn(grad_out, hidden).astype(jnp.bfloat16),
    ]
    return mixed_part, normed_part, weight_parts


def shards_general(
    tokens,
    segments,
    positions,
    cotangent,
    attn_gain,
    ffn_gain,
    w_kv,
    w_query,
    w_out,
    w_gate,
    w_up,
    w_down,
):
    everywhere = ("z", "xc", "mp")
    dp = ("z", "xc")
    z_size = lax.axis_size("z")
    xc_size = lax.axis_size("xc")
    gains = lax.all_gather(
        jnp.stack([attn_gain, ffn_gain], axis=1), everywhere, axis=0, tiled=True
    ).astype(jnp.float32)
    gain_one, gain_two = gains[:, 0], gains[:, 1]
    kv_weight = lax.all_gather(w_kv, everywhere, axis=0, tiled=True)
    head_dim = kv_weight.shape[1] // 2
    width = tokens.shape[1]
    seq_len = segments.shape[0]
    heads_here = w_query.shape[1] // head_dim
    scale = head_dim ** (-0.5)
    cosine, sine = rotary_angles(positions, head_dim)
    inputs_f = tokens.astype(jnp.float32)
    tokens_all = lax.all_gather(tokens, "mp", axis=0, tiled=True)
    normed_one = norm_gain(tokens_all.astype(jnp.float32), gain_one).astype(jnp.bfloat16)
    query_weight = lax.all_gather(w_query, dp, axis=0, tiled=True)
    out_weight = lax.all_gather(w_out, dp, axis=0, tiled=True)

    rows = w_gate.shape[0]
    unit = w_gate.shape[1] // z_size

    def spread(weight):
        pieces = weight.reshape(rows, z_size, unit).transpose(1, 0, 2)
        pieces = lax.all_to_all(pieces, "z", split_axis=0, concat_axis=0, tiled=True)
        return lax.all_gather(pieces, "xc", axis=1, tiled=False).reshape(width, unit)

    gate_weight, up_weight, down_weight = spread(w_gate), spread(w_up), spread(w_down)
    grad_all = lax.all_gather(cotangent, ("z", "mp"), axis=0, tiled=True)

    query = jnp.dot(normed_one, query_weight, preferred_element_type=jnp.float32).reshape(
        seq_len, heads_here, head_dim
    )
    rotated = (rotate(query, cosine[:, None], sine[:, None]) * scale).astype(jnp.bfloat16)
    keyval = jnp.dot(normed_one, kv_weight, preferred_element_type=jnp.float32)
    keys = rotate(keyval[:, :head_dim], cosine, sine).astype(jnp.bfloat16)
    values = keyval[:, head_dim:].astype(jnp.bfloat16)
    allowed = block_allowed(segments, 0, seq_len)
    scores = jnp.einsum("thd,sd->hts", rotated, keys, preferred_element_type=jnp.float32)
    scores = jnp.where(allowed[None], scores, masked_score)
    row_max = jnp.max(scores, axis=-1, keepdims=True)
    weights = jnp.exp(scores - row_max)
    probs = weights / jnp.sum(weights, axis=-1, keepdims=True)
    probs_low = probs.astype(jnp.bfloat16)
    attn_vals = (
        jnp.einsum("hts,sd->thd", probs_low, values, preferred_element_type=jnp.float32)
        .reshape(seq_len, heads_here * head_dim)
        .astype(jnp.bfloat16)
    )
    mid = inputs_f + lax.psum_scatter(
        matmul_nt(attn_vals, out_weight).astype(jnp.bfloat16),
        "mp",
        scatter_dimension=0,
        tiled=True,
    ).astype(jnp.float32)
    normed_two = norm_gain(mid, gain_two).astype(jnp.bfloat16)
    normed_all = lax.all_gather(normed_two, ("z", "mp"), axis=0, tiled=True)

    mixed_part, normed_part, weight_parts = ffn_pass(
        normed_all, grad_all, gate_weight, up_weight, down_weight
    )
    grad_normed_two = lax.psum_scatter(
        normed_part, ("z", "mp"), scatter_dimension=0, tiled=True
    ).astype(jnp.float32)
    mixed = (
        mid
        + lax.psum_scatter(mixed_part, ("z", "mp"), scatter_dimension=0, tiled=True).astype(
            jnp.float32
        )
    ).astype(jnp.bfloat16)

    def collect(part):
        pieces = part.reshape(z_size, xc_size, rows, unit).transpose(1, 0, 2, 3)
        pieces = pieces.reshape(xc_size * z_size * rows, unit)
        pieces = lax.psum_scatter(pieces, "xc", scatter_dimension=0, tiled=True)
        pieces = pieces.reshape(z_size, rows, unit)
        pieces = lax.all_to_all(pieces, "z", split_axis=0, concat_axis=0, tiled=True)
        return pieces.transpose(1, 0, 2).reshape(rows, z_size * unit).astype(jnp.float32)

    w_gate_grad, w_up_grad, w_down_grad = [collect(part) for part in weight_parts]

    norm_pull_two = jax.vjp(norm_gain, mid, gain_two)[1]
    grad_mid_norm, grad_gain_two = norm_pull_two(grad_normed_two)
    grad_mid = cotangent.astype(jnp.float32) + grad_mid_norm
    grad_mid_all = lax.all_gather(grad_mid.astype(jnp.bfloat16), "mp", axis=0, tiled=True)
    grad_vals = (
        jnp.dot(grad_mid_all, out_weight, preferred_element_type=jnp.float32)
        .astype(jnp.bfloat16)
        .reshape(seq_len, heads_here, head_dim)
    )
    grad_probs = jnp.einsum("thd,sd->hts", grad_vals, values, preferred_element_type=jnp.float32)
    delta = jnp.sum(probs * grad_probs, axis=-1, keepdims=True)
    grad_scores = (probs * (grad_probs - delta)).astype(jnp.bfloat16)
    grad_rot = jnp.einsum("hts,sd->thd", grad_scores, keys, preferred_element_type=jnp.float32)
    key_sum = jnp.einsum("hts,thd->sd", grad_scores, rotated, preferred_element_type=jnp.float32)
    value_sum = jnp.einsum("hts,thd->sd", probs_low, grad_vals, preferred_element_type=jnp.float32)
    grad_query = (
        (unrotate(grad_rot, cosine[:, None], sine[:, None]) * scale)
        .reshape(seq_len, heads_here * head_dim)
        .astype(jnp.bfloat16)
    )
    grad_kv = jnp.concatenate([unrotate(key_sum, cosine, sine), value_sum], axis=1).astype(
        jnp.bfloat16
    )
    grad_normed_one = lax.psum_scatter(
        (matmul_nt(grad_query, query_weight) + matmul_nt(grad_kv, kv_weight)).astype(jnp.bfloat16),
        "mp",
        scatter_dimension=0,
        tiled=True,
    ).astype(jnp.float32)
    norm_pull_one = jax.vjp(norm_gain, inputs_f, gain_one)[1]
    grad_input_norm, grad_gain_one = norm_pull_one(grad_normed_one)
    tokens_grad = (grad_mid + grad_input_norm).astype(jnp.bfloat16)

    w_query_grad = lax.psum_scatter(
        matmul_tn(normed_one, grad_query).astype(jnp.bfloat16), dp, scatter_dimension=0, tiled=True
    ).astype(jnp.float32)
    w_out_grad = lax.psum_scatter(
        matmul_tn(grad_mid_all, attn_vals).astype(jnp.bfloat16), dp, scatter_dimension=0, tiled=True
    ).astype(jnp.float32)
    small = jnp.concatenate(
        [matmul_tn(normed_one, grad_kv), grad_gain_one[:, None], grad_gain_two[:, None]], axis=1
    )
    small = lax.psum_scatter(small, everywhere, scatter_dimension=0, tiled=True)
    kv_grad = small[:, : 2 * head_dim]
    return (
        mixed,
        tokens_grad,
        small[:, 2 * head_dim],
        small[:, 2 * head_dim + 1],
        kv_grad,
        w_query_grad,
        w_out_grad,
        w_gate_grad,
        w_up_grad,
        w_down_grad,
    )


def shards_fast(
    tokens,
    segments,
    positions,
    cotangent,
    attn_gain,
    ffn_gain,
    w_kv,
    w_query,
    w_out,
    w_gate,
    w_up,
    w_down,
):
    seq_len = segments.shape[0]
    cosine, sine = rotary_angles(positions, w_kv.shape[1] // 2)
    table = jnp.stack(
        [
            jnp.concatenate([cosine, cosine], axis=1),
            jnp.concatenate([-sine, sine], axis=1),
        ]
    )
    gain_rows = jnp.pad(
        jnp.stack([attn_gain, ffn_gain]).astype(jnp.float32),
        ((0, 6), (0, 128 - attn_gain.shape[0])),
    )
    segment_rows = jnp.broadcast_to(segments.astype(jnp.float32)[None, :], (8, seq_len))
    (
        normed_one,
        rotated,
        keys,
        values,
        attn_vals,
        mid,
        normed_two,
        gains,
        allowed,
        kv_weight,
        query_weight,
        out_weight,
        ffn_weights,
        grad_all,
    ) = pre_call(
        tokens,
        w_kv,
        gain_rows,
        table,
        segment_rows,
        cotangent,
        w_query,
        w_out,
        (w_gate, w_up, w_down),
    )
    main = ragged_split(w_gate.shape[1], lax.axis_size("z"))[0]
    grad_mid, gain_part, mix_parts, ffn_sums, grad_mid_low = ffn_call(
        gains, normed_two, grad_all, ffn_weights, mid, w_gate.shape[0], main
    )
    mixed, tokens_grad, gain_grads, kv_grad, query_grad, out_grad, ffn_grads = post_call(
        tokens,
        gains,
        gain_part,
        normed_one,
        rotated,
        keys,
        values,
        attn_vals,
        table,
        allowed,
        kv_weight,
        query_weight,
        out_weight,
        mix_parts,
        grad_mid,
        grad_mid_low,
        mid,
        ffn_sums,
        main,
    )
    *ffn_out, query_grad, out_grad, kv_grad, mixed, tokens_grad = layout_call(
        ffn_sums,
        ffn_grads,
        query_grad,
        out_grad,
        kv_grad,
        mixed,
        tokens_grad,
        w_gate.shape[1],
    )
    share = attn_gain.shape[0]
    place = lax.axis_index(("z", "x", "c", "mp")) * share
    gain_grads = gain_grads.reshape(2, gain_grads.size // 2)
    gain_grads = lax.dynamic_slice(gain_grads, (0, place), (2, share))
    return (
        mixed,
        tokens_grad,
        gain_grads[0],
        gain_grads[1],
        kv_grad,
        query_grad,
        out_grad,
        *ffn_out,
    )


def solution(mesh):
    dp_size, mp_size = mesh.shape["dp"], mesh.shape["mp"]
    if dp_size == 4 * FF_SPLIT and mp_size == 2:
        body, dp = shards_fast, ("z", "x", "c")
        sizes = (FF_SPLIT, 2, 2, mp_size)
    else:
        body, dp = shards_general, ("z", "xc")
        sizes = (FF_SPLIT, dp_size // FF_SPLIT, mp_size)
    all_axes = (*dp, "mp")
    fine = jax.sharding.Mesh(mesh.devices.reshape(sizes), all_axes)
    in_specs = (
        P(all_axes, None),
        P(dp),
        P(dp),
        P(all_axes, None),
        P(all_axes),
        P(all_axes),
        P(all_axes, None),
        P(dp, "mp"),
        P(dp, "mp"),
        P(dp, "mp"),
        P(dp, "mp"),
        P(dp, "mp"),
    )
    out_specs = (
        P(all_axes, None),
        P(all_axes, None),
        P(all_axes),
        P(all_axes),
        P(all_axes, None),
        P(dp, "mp"),
        P(dp, "mp"),
        P(dp, "mp"),
        P(dp, "mp"),
        P(dp, "mp"),
    )
    return jax.shard_map(body, mesh=fine, in_specs=in_specs, out_specs=out_specs, check_vma=False)
```

```python
import functools

import jax
import jax.numpy as jnp
from jax import lax
from jax.experimental import pallas as pl
from jax.experimental.pallas import tpu as pltpu
from jax.sharding import PartitionSpec as P

WINDOW = 2048


epsilon = 1e-06
rope_base = 10000.0
masked_score = -1e30
VMEM_BYTES = 66_000_000


def norm_gain(values, gain):
    return values * lax.rsqrt(jnp.mean(values * values, axis=-1, keepdims=True) + epsilon) * gain


def rotary_angles(positions, head_width):
    quarter = head_width // 4
    freqs = rope_base ** (-jnp.arange(quarter).astype(jnp.float32) / quarter)
    phase = positions.astype(jnp.float32)[:, None] * freqs[None, :]
    return (jnp.cos(phase), jnp.sin(phase))


def rotate(values, cosine, sine):
    quarter = cosine.shape[-1]
    first_half = values[..., :quarter]
    second_half = values[..., quarter : 2 * quarter]
    return jnp.concatenate(
        [
            first_half * cosine - second_half * sine,
            second_half * cosine + first_half * sine,
            values[..., 2 * quarter :],
        ],
        axis=-1,
    )


def unrotate(values, cosine, sine):
    quarter = cosine.shape[-1]
    first_half = values[..., :quarter]
    second_half = values[..., quarter : 2 * quarter]
    return jnp.concatenate(
        [
            first_half * cosine + second_half * sine,
            second_half * cosine - first_half * sine,
            values[..., 2 * quarter :],
        ],
        axis=-1,
    )


def gelu_product(gate, up_proj):
    return jax.nn.gelu(gate, approximate=True) * up_proj


def matmul_nt(left, right):
    return lax.dot_general(
        left, right, (((1,), (1,)), ((), ())), preferred_element_type=jnp.float32
    )


def matmul_tn(left, right):
    return lax.dot_general(
        left, right, (((0,), (0,)), ((), ())), preferred_element_type=jnp.float32
    )


def block_allowed(segments, first_row, rows):
    seq_len = segments.shape[0]
    query_rows = first_row + jnp.arange(rows)
    key_rows = jnp.arange(seq_len)
    return (
        (segments[:, None] == segments[None, :])
        & (key_rows[None, :] <= query_rows[:, None])
        & (query_rows[:, None] - key_rows[None, :] < WINDOW)
    )


MESH_ID = pl.DeviceIdType.MESH
GELU_A = 0.7978845608028654
GELU_B = 0.044715
TILE = 256
WIDE = 512


def remote(src, dst, send_sem, recv_sem, where):
    return pltpu.make_async_remote_copy(
        src_ref=src,
        dst_ref=dst,
        send_sem=send_sem,
        recv_sem=recv_sem,
        device_id=where,
        device_id_type=MESH_ID,
    )


def dot_nn(left, right):
    return lax.dot_general(
        left, right, (((1,), (0,)), ((), ())), preferred_element_type=jnp.float32
    )


def gelu_parts(gate):
    square = gate * gate
    bend = jnp.tanh(GELU_A * gate * (1.0 + GELU_B * square))
    half = 0.5 * (1.0 + bend)
    slope = half + 0.5 * gate * (1.0 - bend * bend) * GELU_A * (1.0 + 3.0 * GELU_B * square)
    return gate * half, slope


def add_rows(first, rest, out, count):
    def body(index, carry):
        step = pl.ds(pl.multiple_of(index * 32, 32), 32)
        total = first[step, :].astype(jnp.float32)
        for other in rest:
            total = total + other[step, :].astype(jnp.float32)
        out[step, :] = total.astype(out.dtype)
        return carry

    lax.fori_loop(0, count // 32, body, 0)


def norm_back(values, gain, upstream):
    scale = lax.rsqrt(jnp.mean(values * values, axis=-1, keepdims=True) + epsilon)
    normed = values * scale
    pulled = gain * upstream
    back = scale * (pulled - normed * jnp.mean(normed * pulled, axis=-1, keepdims=True))
    return back, jnp.sum(upstream * normed, axis=0, keepdims=True)


def ffn_kernel(
    z_size,
    main,
    gain_ref,
    own_hbm,
    dy_hbm,
    w_hbm,
    mid_hbm,
    gm_ref,
    gain_part,
    mix_hbm,
    sums_hbm,
    gm_hbm,
    n2,
    dy,
    w3,
    h3,
    n2_t,
    dy_t,
    gn_part,
    mix_buf,
    gn_y,
    gn_z,
    gn_s,
    c_in,
    x_in,
    mid,
    load_sem,
    mix_sem,
    ag_y_send,
    ag_y_recv,
    ag_z_send,
    ag_z_recv,
    rs_y_send,
    rs_y_recv,
    rs_z_send,
    rs_z_recv,
    c_send,
    c_recv,
    x_send,
    x_recv,
    out_sem,
):
    own = own_hbm.shape[0] // 2
    width = own_hbm.shape[1]
    units = w3.shape[2]
    rows = c_in.shape[3]
    span = width // z_size
    me_y, me_z = lax.axis_index("mp"), lax.axis_index("z")
    me_x, me_c = lax.axis_index("x"), lax.axis_index("c")
    mine = pl.ds(pl.multiple_of(me_y * own, own), own)
    theirs = pl.ds(pl.multiple_of((1 - me_y) * own, own), own)
    to_y, to_x, to_c = {"mp": 1 - me_y}, {"x": 1 - me_x}, {"c": 1 - me_c}

    def ahead(step):
        return lax.rem(me_z + step, z_size)

    def to_z(step):
        return {"z": ahead(step)}

    def row_block(z_at, x_at, c_at):
        return pl.ds(pl.multiple_of(((z_at * 2 + x_at) * 2 + c_at) * rows, rows), rows)

    inner = (me_z > 0) & (me_z < z_size - 1)
    outer = (me_z == 0) | (me_z == z_size - 1)

    def w_load(index, columns):
        cols = pl.ds(0, columns)
        return pltpu.make_async_copy(
            w_hbm.at[index, :, cols], w3.at[index, :, cols], load_sem.at[z_size + index]
        )

    def w_loads(act):
        for case, columns in ((inner, units), (outer, main)):

            @pl.when(case)
            def _(columns=columns):
                for index in range(3):
                    act(w_load(index, columns))

    w_loads(lambda copy: copy.start())
    dy_loads = [
        pltpu.make_async_copy(dy_hbm.at[index], dy, load_sem.at[index])
        for index in range(z_size)
    ]
    own_load = pltpu.make_async_copy(own_hbm, n2.at[0], load_sem.at[z_size + 3])
    mid_load = pltpu.make_async_copy(mid_hbm, mid, load_sem.at[z_size + 4])
    for load in (own_load, dy_loads[0], mid_load):
        load.start()

    barrier = pltpu.get_barrier_semaphore()
    peers = [to_y, to_x, to_c] + [to_z(step) for step in range(1, z_size)]
    for where in peers:
        pl.semaphore_signal(barrier, inc=1, device_id=where, device_id_type=MESH_ID)
    pl.semaphore_wait(barrier, len(peers))

    def ag_y(index):
        block = n2.at[index, mine]
        return remote(block, block, ag_y_send.at[index], ag_y_recv.at[index], to_y)

    def ag_y_in(index):
        block = n2.at[index, theirs]
        return remote(block, block, ag_y_send.at[index], ag_y_recv.at[index], to_y)

    def ag_z(index):
        src = own_hbm.at[mine] if index == 0 else n2.at[index, mine]
        return remote(
            src, n2.at[index + 1, mine], ag_z_send.at[index], ag_z_recv.at[index + 1], to_z(1)
        )

    def ag_z_in(index):
        block = n2.at[index, mine]
        return remote(block, block, ag_z_send.at[0], ag_z_recv.at[index], to_z(1))

    def ag_last():
        return remote(
            n2.at[2, theirs], n2.at[3, theirs], ag_y_send.at[3], ag_y_recv.at[3], to_z(1)
        )

    def forward(index):
        ag_z_in(index).wait_recv()
        ag_z(index).start()
        ag_y(index).start()

    ag_z(0).start()

    mix_copies = []

    def turn(source, target, index):
        def turn_tile(tile, carry):
            at = pl.ds(pl.multiple_of(tile * span, 128), span)
            target[at, pl.ds(index * 2 * own, 2 * own)] = source[:, at].T
            return carry

        lax.fori_loop(0, z_size, turn_tile, 0)

    def chunk(index):
        if index:
            mix_copies[index - 1].wait()
        dy_loads[index].wait()
        rows_at = pl.ds(index * 2 * own, 2 * own)

        def up_tile(tile, carry):
            cols = pl.ds(pl.multiple_of(tile * TILE, TILE), TILE)
            gate = dot_nn(n2[index], w3[0, :, cols])
            up_proj = dot_nn(n2[index], w3[1, :, cols])
            grad_hidden = dot_nn(dy[...], w3[2, :, cols])
            act, slope = gelu_parts(gate)
            h3[0, rows_at, cols] = (grad_hidden * up_proj * slope).astype(jnp.bfloat16)
            h3[1, rows_at, cols] = (grad_hidden * act).astype(jnp.bfloat16)
            h3[2, rows_at, cols] = (act * up_proj).astype(jnp.bfloat16)
            return carry

        lax.fori_loop(0, units // TILE, up_tile, 0)

        def down_tile(tile, carry):
            at = pl.ds(pl.multiple_of(tile * span, 128), span)
            normed = matmul_nt(w3[0, at, :], h3[0, rows_at, :]) + matmul_nt(
                w3[1, at, :], h3[1, rows_at, :]
            )
            mixed = matmul_nt(w3[2, at, :], h3[2, rows_at, :])
            for half in range(2):
                cols = slice(half * own, (half + 1) * own)
                gn_part[index, half, at, :] = normed[:, cols].astype(jnp.bfloat16)
                mix_buf[half, at, :] = mixed[:, cols].astype(jnp.bfloat16)
            return carry

        lax.fori_loop(0, z_size, down_tile, 0)
        copy = pltpu.make_async_copy(mix_buf, mix_hbm.at[index], mix_sem.at[index])
        copy.start()
        mix_copies.append(copy)
        if index:
            rs_y(index).start()
        turn(n2.at[index], n2_t, index)
        turn(dy, dy_t, index)
        if index + 1 < z_size:
            dy_loads[index + 1].start()

    def rs_y(index):
        return remote(
            gn_part.at[index, 1 - me_y], gn_y.at[index], rs_y_send.at[index], rs_y_recv.at[index], to_y
        )

    def rs_z(index):
        return remote(
            gn_s.at[index - 1],
            gn_z.at[index - 1],
            rs_z_send.at[index],
            rs_z_recv.at[index - 1],
            to_z(1),
        )

    def rs_step(index):
        rs_y(index).wait_recv()
        slot = (index - 2) % z_size
        if index != 1:
            remote(
                gn_s.at[slot], gn_z.at[slot], rs_z_send.at[1], rs_z_recv.at[slot], to_z(1)
            ).wait_recv()

        def add_tile(tile, carry):
            at = pl.ds(pl.multiple_of(tile * TILE, TILE), TILE)
            total = gn_part[index, me_y, at, :].astype(jnp.float32) + gn_y[index, at, :].astype(
                jnp.float32
            )
            if index != 1:
                total = total + gn_z[slot, at, :].astype(jnp.float32)
            if index == 0:
                gm_ref[:, at] = total.T
            else:
                gn_s[index - 1, at, :] = total.astype(jnp.bfloat16)
            return carry

        lax.fori_loop(0, width // TILE, add_tile, 0)
        if index != 0:
            rs_z(index).start()


    def grads(step):
        at = pl.ds(pl.multiple_of(ahead(step) * span, 128), span)
        for kind, source in enumerate((n2_t, n2_t, dy_t)):

            def tile_body(tile, carry, kind=kind, source=source):
                cols = pl.ds(pl.multiple_of(tile * WIDE, WIDE), WIDE)
                w3[kind, at, cols] = dot_nn(source[at, :], h3[kind, :, cols]).astype(jnp.bfloat16)
                return carry

            lax.fori_loop(0, units // WIDE, tile_body, 0)
        for far in (1, 0):
            for kind in range(3):
                over_c(kind, step, far).start()

    def over_c(kind, step, far):
        x_at = 1 - me_x if far else me_x
        return remote(
            w3.at[kind, row_block(ahead(step), x_at, 1 - me_c)],
            c_in.at[kind, step, far],
            c_send.at[kind, step, far],
            c_recv.at[kind, step, far],
            to_c,
        )

    def over_x(kind):
        return remote(
            w3.at[kind, row_block(ahead(1), 1 - me_x, me_c)],
            x_in.at[kind],
            x_send.at[kind],
            x_recv.at[kind],
            to_x,
        )

    out_copies = []

    def keep(kind, step, far, block):
        copy = pltpu.make_async_copy(
            block, sums_hbm.at[kind, step, far], out_sem.at[kind, step, far]
        )
        copy.start()
        out_copies.append(copy)

    def core_sums(step):
        for far in (1, 0):
            for kind in range(3):
                over_c(kind, step, far).wait_recv()
                x_at = 1 - me_x if far else me_x
                block = w3.at[kind, row_block(ahead(step), x_at, me_c)]
                add_rows(block, [c_in.at[kind, step, far]], block, rows)
                if step != 1:
                    keep(kind, step, far, block)
                elif far:
                    over_x(kind).start()

    def first_sums():
        for kind in range(3):
            over_x(kind).wait_recv()
            block = w3.at[kind, row_block(ahead(1), me_x, me_c)]
            add_rows(block, [x_in.at[kind]], block, rows)
            keep(kind, 1, 0, block)

    own_load.wait()
    w_loads(lambda copy: copy.wait())

    @pl.when(outer)
    def _():
        w3[:, :, main:] = jnp.zeros((3, width, units - main), jnp.bfloat16)

    chunk(0)
    forward(1)
    forward(2)
    ag_y_in(1).wait_recv()
    chunk(1)
    ag_y_in(2).wait_recv()
    ag_last().start()
    chunk(2)
    rs_step(1)
    ag_z_in(3).wait_recv()
    ag_last().wait_recv()
    chunk(3)
    rs_y(0).start()
    rs_step(2)
    grads(1)
    grads(2)
    core_sums(1)
    rs_step(3)
    grads(3)
    core_sums(2)
    grads(0)
    core_sums(3)
    rs_step(0)
    core_sums(0)

    cot_load = pltpu.make_async_copy(
        dy_hbm.at[0, mine], dy.at[pl.ds(0, own)], load_sem.at[z_size + 3]
    )
    cot_load.start()
    cot_load.wait()
    mid_load.wait()

    def mid_rows(index, total):
        at = pl.ds(pl.multiple_of(index * 32, 32), 32)
        grad, gain_sum = norm_back(mid[at, :], gain_ref[1:2, :], gm_ref[at, :])
        grad = grad + dy[at, :].astype(jnp.float32)
        gm_ref[at, :] = grad
        dy[pl.ds(pl.multiple_of(own + index * 32, 32), 32), :] = grad.astype(jnp.bfloat16)
        return total + gain_sum

    gain_sum = lax.fori_loop(0, own // 32, mid_rows, jnp.zeros((1, width), jnp.float32))
    gm_save = pltpu.make_async_copy(dy.at[pl.ds(own, own)], gm_hbm, load_sem.at[z_size + 3])
    gm_save.start()
    for index in range(4):
        gain_part[index : index + 1, :] = jnp.zeros((1, span), jnp.float32)
        gain_part[4 + index : 5 + index, :] = gain_sum[:, index * span : (index + 1) * span]
    first_sums()
    gm_save.wait()

    for copy in mix_copies[3:] + out_copies:
        copy.wait()
    for index in range(z_size):
        if index in (1, 2):
            ag_y(index).wait_send()
        if index == 3:
            ag_last().wait_send()
        rs_y(index).wait_send()
        if index < z_size - 1:
            ag_z(index).wait_send()
        if index:
            rs_z(index).wait_send()
        for kind in range(3):
            over_c(kind, index, 0).wait_send()
            over_c(kind, index, 1).wait_send()
            if index == 1:
                over_x(kind).wait_send()


def ffn_call(gains, normed, grad_all, weights, mid, rows, main):
    z_size = lax.axis_size("z")
    pair, width = normed.shape
    units = weights.shape[2]
    own = pair // 2
    wide = lambda *lead: pltpu.VMEM((*lead, width), jnp.bfloat16)
    tall = lambda *lead: pltpu.VMEM((*lead, width, own), jnp.bfloat16)
    dma = lambda *lead: pltpu.SemaphoreType.DMA(lead)
    vmem = pl.BlockSpec(memory_space=pltpu.VMEM)
    hbm = pl.BlockSpec(memory_space=pl.ANY)
    return pl.pallas_call(
        functools.partial(ffn_kernel, z_size, main),
        out_shape=(
            jax.ShapeDtypeStruct((own, width), jnp.float32),
            jax.ShapeDtypeStruct((8, width // z_size), jnp.float32),
            jax.ShapeDtypeStruct((z_size, 2, width, own), jnp.bfloat16),
            jax.ShapeDtypeStruct((3, z_size, 2, rows, units), jnp.bfloat16),
            jax.ShapeDtypeStruct((own, width), jnp.bfloat16),
        ),
        in_specs=[vmem, hbm, hbm, hbm, hbm],
        out_specs=(vmem, vmem, hbm, hbm, hbm),
        scratch_shapes=[
            wide(z_size, pair),
            wide(pair),
            pltpu.VMEM(weights.shape, jnp.bfloat16),
            pltpu.VMEM((3, z_size * pair, units), jnp.bfloat16),
            pltpu.VMEM((width, z_size * pair), jnp.bfloat16),
            pltpu.VMEM((width, z_size * pair), jnp.bfloat16),
            tall(z_size, 2),
            tall(2),
            tall(z_size),
            tall(z_size - 1),
            tall(z_size - 1),
            pltpu.VMEM((3, z_size, 2, rows, units), jnp.bfloat16),
            pltpu.VMEM((3, rows, units), jnp.bfloat16),
            pltpu.VMEM((own, width), jnp.float32),
            dma(z_size + 5),
            dma(z_size),
            dma(z_size),
            dma(z_size),
            dma(z_size),
            dma(z_size),
            dma(z_size),
            dma(z_size),
            dma(z_size),
            dma(z_size),
            dma(3, z_size, 2),
            dma(3, z_size, 2),
            dma(3),
            dma(3),
            dma(3, z_size, 2),
        ],
        compiler_params=pltpu.CompilerParams(
            collective_id=0, has_side_effects=True, vmem_limit_bytes=VMEM_BYTES
        ),
        cost_estimate=pl.CostEstimate(
            flops=18 * z_size * pair * width * units,
            bytes_accessed=4 * weights.size + 12 * z_size * pair * width,
            transcendentals=z_size * pair * units,
        ),
    )(gains, normed, grad_all, weights, mid)


def spin(values, table):
    first = values[:, : values.shape[1] // 2]
    turned = first * table[0] + pltpu.roll(first, first.shape[1] // 2, 1) * table[1]
    return jnp.concatenate([turned, values[:, values.shape[1] // 2 :]], axis=1)


def spin_back(values, table):
    first = values[:, : values.shape[1] // 2]
    turned = first * table[0] - pltpu.roll(first, first.shape[1] // 2, 1) * table[1]
    return jnp.concatenate([turned, values[:, values.shape[1] // 2 :]], axis=1)


def head_probs(rotated, keys, allowed):
    scores = jnp.where(allowed > 0.5, matmul_nt(rotated, keys), masked_score)
    weights = jnp.exp(scores - jnp.max(scores, axis=-1, keepdims=True))
    return weights / jnp.sum(weights, axis=-1, keepdims=True)


def ragged_split(columns, parts):
    main = columns // parts // 128 * 128
    return main, main + 128


def pre_kernel(
    z_size,
    tok_ref,
    wkv_ref,
    gains_ref,
    table_ref,
    seg_ref,
    cot_hbm,
    wq_hbm,
    wo_hbm,
    wg_hbm,
    wu_hbm,
    wd_hbm,
    n1_ref,
    rot_ref,
    key_ref,
    val_ref,
    att_ref,
    mid_ref,
    n2_ref,
    gain_ref,
    allow_ref,
    kv_out,
    wq_out,
    wo_out,
    w3_out,
    dy_out,
    kv_w,
    q_w,
    o_w,
    tok,
    part,
    part_y,
    query,
    y_send,
    y_recv,
    ky_send,
    ky_recv,
    az_send,
    az_recv,
    ax_send,
    ax_recv,
    ac_send,
    ac_recv,
    fz_send,
    fz_recv,
    fx_send,
    fx_recv,
    fc_send,
    fc_recv,
    dz_send,
    dz_recv,
    dy_send,
    dy_recv,
    local_sem,
):
    me_z, me_x = lax.axis_index("z"), lax.axis_index("x")
    me_c, me_y = lax.axis_index("c"), lax.axis_index("mp")
    own, width = tok_ref.shape
    rows = wq_hbm.shape[0]
    half_rows = wkv_ref.shape[0]
    head = key_ref.shape[1]
    main, units = ragged_split(wg_hbm.shape[1], z_size)
    to_y, to_x, to_c = {"mp": 1 - me_y}, {"x": 1 - me_x}, {"c": 1 - me_c}

    def to_z(step):
        return {"z": lax.rem(me_z + step, z_size)}

    def from_z(step):
        return lax.rem(me_z - step + z_size, z_size)

    def row_block(step, x_at, c_at):
        start = ((from_z(step) * 2 + x_at) * 2 + c_at) * rows
        return pl.ds(pl.multiple_of(start, rows), rows)

    mine = pl.ds(pl.multiple_of(me_y * own, own), own)
    theirs = pl.ds(pl.multiple_of((1 - me_y) * own, own), own)
    bufs = (kv_w, q_w, o_w)
    inputs = (None, wq_hbm, wo_hbm)

    locals_ = []

    def local(src, dst):
        copy = pltpu.make_async_copy(src, dst, local_sem.at[len(locals_)])
        copy.start()
        locals_.append(copy)
        return copy

    here = row_block(0, me_x, me_c)
    own_q = local(wq_hbm, q_w.at[here])
    own_o = local(wo_hbm, o_w.at[here])
    ffn_in = (wg_hbm, wu_hbm, wd_hbm)

    def body_of(target):
        return pl.ds(pl.multiple_of(target * main, 128), main), pl.ds(0, main)

    def tail_of(target):
        start = z_size * main + lax.rem(target + 1, 2) * 128
        return pl.ds(pl.multiple_of(start, 128), 128), pl.ds(main, 128)

    def is_inner(at):
        return (at > 0) & (at < z_size - 1)

    own_f = []
    for kind in range(3):
        src, dst = body_of(me_z)
        own_f.append(local(ffn_in[kind].at[:, src], w3_out.at[kind, here, dst]))

    def own_tail(kind):
        src, dst = tail_of(me_z)
        return pltpu.make_async_copy(
            ffn_in[kind].at[:, src], w3_out.at[kind, here, dst], local_sem.at[12 + kind]
        )

    @pl.when(is_inner(me_z))
    def _():
        for kind in range(3):
            own_tail(kind).start()
    own_d = local(cot_hbm, dy_out.at[0, mine])

    kv_own = pl.ds(pl.multiple_of(here.start + me_y * half_rows, half_rows), half_rows)
    spread = jnp.concatenate([gains_ref[...], jnp.zeros((120, 128), jnp.float32)], axis=0).T
    kv_w[kv_own, : 2 * head] = wkv_ref[...]
    kv_w[kv_own, 2 * head :] = spread[:half_rows, :].astype(jnp.bfloat16)

    barrier = pltpu.get_barrier_semaphore()
    peers = [to_y, to_x, to_c] + [to_z(step) for step in range(1, z_size)]
    for where in peers:
        pl.semaphore_signal(barrier, inc=1, device_id=where, device_id_type=MESH_ID)
    pl.semaphore_wait(barrier, len(peers))

    tok_y = remote(tok_ref, tok.at[mine], y_send.at[1], y_recv.at[1], to_y)
    tok_y_in = remote(tok_ref, tok.at[theirs], y_send.at[1], y_recv.at[1], to_y)
    part_out = remote(part.at[theirs], part_y, y_send.at[2], y_recv.at[2], to_y)
    n2_y = remote(n2_ref.at[mine], n2_ref.at[mine], y_send.at[3], y_recv.at[3], to_y)
    n2_y_in = remote(n2_ref.at[theirs], n2_ref.at[theirs], y_send.at[3], y_recv.at[3], to_y)

    def block_of(kind, step, x_at):
        if kind:
            return row_block(step, x_at, me_c)
        return kv_rows(step, x_at, me_y)

    def kv_rows(step, x_at, y_at):
        start = row_block(step, x_at, me_c).start + y_at * half_rows
        return pl.ds(pl.multiple_of(start, half_rows), half_rows)

    def kv_y(step, far):
        x_at = 1 - me_x if far else me_x
        block = kv_w.at[kv_rows(step, x_at, me_y)]
        slot = step + z_size * far
        return remote(block, block, ky_send.at[slot], ky_recv.at[slot], to_y)

    def kv_y_in(step, far):
        x_at = 1 - me_x if far else me_x
        block = kv_w.at[kv_rows(step, x_at, 1 - me_y)]
        slot = step + z_size * far
        return remote(block, block, ky_send.at[slot], ky_recv.at[slot], to_y)

    def source(kind, step):
        if isinstance(step, int) and step == 0 and kind:
            return inputs[kind]
        return bufs[kind].at[block_of(kind, step, me_x)]

    first_z, last_z = (z_size - 1 - me_z) // (z_size - 1), me_z // (z_size - 1)
    inner = first_z + last_z == 0
    order = (0, 1 + 2 * first_z, 3 - first_z - last_z, 2 - first_z + last_z)
    hops = (
        None,
        (lax.rem(me_z + 1, z_size), 2),
        (lax.rem(me_z + z_size - 1, z_size), 2),
        (lax.rem(3 * (me_z + 3), z_size), lax.rem(2 * me_z + 3, z_size)),
    )

    def a_z_own(kind, right):
        return remote(
            source(kind, 0),
            bufs[kind].at[block_of(kind, 0, me_x)],
            az_send.at[kind, right],
            az_recv.at[kind, 1 if right else z_size - 1],
            to_z(1 if right else z_size - 1),
        )

    def a_z_start(kind):
        @pl.when(last_z == 0)
        def _():
            a_z_own(kind, 1).start()

        @pl.when(first_z == 0)
        def _():
            a_z_own(kind, 0).start()

    def a_z(kind, index):
        target, slot = hops[index]
        block = bufs[kind].at[block_of(kind, order[index], me_x)]
        return remote(
            block, block, az_send.at[kind, 1 + index], az_recv.at[kind, slot], {"z": target}
        )

    def a_z_next(kind, index):
        @pl.when(inner)
        def _():
            a_z(kind, index).start()

    def a_z_done(kind):
        @pl.when(last_z == 0)
        def _():
            a_z_own(kind, 1).wait_send()

        @pl.when(first_z == 0)
        def _():
            a_z_own(kind, 0).wait_send()

        @pl.when(inner)
        def _():
            for index in range(1, z_size):
                a_z(kind, index).wait_send()

    def a_z_in(kind, step):
        block = bufs[kind].at[block_of(kind, step, me_x)]
        return remote(block, block, az_send.at[kind, 0], az_recv.at[kind, step], to_z(1))

    def a_x(kind, step):
        return remote(
            source(kind, step),
            bufs[kind].at[block_of(kind, step, me_x)],
            ax_send.at[kind, step],
            ax_recv.at[kind, step],
            to_x,
        )

    def a_x_in(kind, step):
        block = bufs[kind].at[block_of(kind, step, 1 - me_x)]
        return remote(block, block, ax_send.at[kind, step], ax_recv.at[kind, step], to_x)

    def a_c(kind, step, far):
        x_at = 1 - me_x if far else me_x
        block = bufs[kind].at[row_block(step, x_at, me_c)]
        src = source(kind, step) if kind and not far else block
        slot = step + z_size * far
        return remote(src, block, ac_send.at[kind, slot], ac_recv.at[kind, slot], to_c)

    def a_c_in(kind, step, far):
        x_at = 1 - me_x if far else me_x
        block = bufs[kind].at[row_block(step, x_at, 1 - me_c)]
        slot = step + z_size * far
        return remote(block, block, ac_send.at[kind, slot], ac_recv.at[kind, slot], to_c)

    def f_z(kind, step, act):
        target = lax.rem(me_z + step, z_size)

        def piece(index, src, dst):
            return remote(
                ffn_in[kind].at[:, src],
                w3_out.at[kind, here, dst],
                fz_send.at[kind, step, index],
                fz_recv.at[kind, step, index],
                to_z(step),
            )

        act(piece(0, *body_of(target)))

        @pl.when(is_inner(target))
        def _():
            act(piece(1, *tail_of(target)))

    def f_z_wait(kind, step):
        block = row_block(step, me_x, me_c)

        def piece(index, dst):
            part = w3_out.at[kind, block, dst]
            return remote(
                part, part, fz_send.at[kind, step, index], fz_recv.at[kind, step, index], to_z(step)
            )

        piece(0, pl.ds(0, main)).wait_recv()

        @pl.when(inner)
        def _():
            piece(1, pl.ds(main, 128)).wait_recv()

    def f_x(kind, step, x_at, act):
        for case, columns in ((inner, units), (first_z + last_z > 0, main)):

            @pl.when(case)
            def _(columns=columns):
                block = w3_out.at[kind, row_block(step, x_at, me_c), pl.ds(0, columns)]
                act(remote(block, block, fx_send.at[kind, step], fx_recv.at[kind, step], to_x))

    def f_x_start(kind, step):
        f_x(kind, step, me_x, lambda copy: copy.start())

    def f_x_wait(kind, step):
        f_x(kind, step, 1 - me_x, lambda copy: copy.wait_recv())

    def f_x_done(kind, step):
        f_x(kind, step, me_x, lambda copy: copy.wait_send())

    def f_c(kind, step, far):
        block = w3_out.at[kind, row_block(step, 1 - me_x if far else me_x, me_c)]
        slot = step + z_size * far
        return remote(block, block, fc_send.at[kind, slot], fc_recv.at[kind, slot], to_c)

    def f_c_in(kind, step, far):
        block = w3_out.at[kind, row_block(step, 1 - me_x if far else me_x, 1 - me_c)]
        slot = step + z_size * far
        return remote(block, block, fc_send.at[kind, slot], fc_recv.at[kind, slot], to_c)

    def d_source(step):
        return cot_hbm if isinstance(step, int) else dy_out.at[step, mine]

    def d_z_own(right):
        slot = 1 if right else z_size - 1
        return remote(
            cot_hbm, dy_out.at[slot, mine], dz_send.at[right], dz_recv.at[slot], to_z(slot)
        )

    def d_z_start():
        @pl.when(last_z == 0)
        def _():
            d_z_own(1).start()

        @pl.when(first_z == 0)
        def _():
            d_z_own(0).start()

    def d_z(index):
        target, slot = hops[index]
        return remote(
            dy_out.at[order[index], mine],
            dy_out.at[slot, mine],
            dz_send.at[1 + index],
            dz_recv.at[slot],
            {"z": target},
        )

    def d_z_done():
        @pl.when(last_z == 0)
        def _():
            d_z_own(1).wait_send()

        @pl.when(first_z == 0)
        def _():
            d_z_own(0).wait_send()

        @pl.when(inner)
        def _():
            for index in range(1, z_size):
                d_z(index).wait_send()

    def d_z_in(step):
        block = dy_out.at[step, mine]
        return remote(block, block, dz_send.at[0], dz_recv.at[step], to_z(1))

    def d_y(step):
        return remote(
            d_source(step), dy_out.at[step, mine], dy_send.at[step], dy_recv.at[step], to_y
        )

    def d_y_in(step):
        block = dy_out.at[step, theirs]
        return remote(block, block, dy_send.at[step], dy_recv.at[step], to_y)

    for kind in (1, 0, 2):
        a_z_start(kind)
        a_x(kind, 0).start()
    kv_y(0, 0).start()
    tok_y.start()
    for kind in (1, 2):
        a_c(kind, 0, 0).start()

    for at_end, away in ((first_z, 1), (last_z, z_size - 1)):

        @pl.when(at_end > 0)
        def _(away=away):
            for kind in range(3):
                f_z(kind, away, lambda copy: copy.start())

    tok[mine, :] = tok_ref[...]
    seq = 2 * own
    query_at = lax.broadcasted_iota(jnp.int32, (seq, seq), 0)
    key_at = lax.broadcasted_iota(jnp.int32, (seq, seq), 1)
    same = seg_ref[...].T[:, :1] == seg_ref[:1, :]
    allowed = same & (key_at <= query_at) & (query_at - key_at < WINDOW)
    allow_ref[...] = jnp.where(allowed, 1.0, 0.0)
    d_y(0).start()

    def from_x(index):
        step = order[index]
        for kind in (1, 0, 2):
            a_x_in(kind, step).wait_recv()
            if kind:
                a_c(kind, step, 1).start()
            else:
                kv_y(step, 1).start()

    def from_y(index):
        step = order[index]
        for far in range(2):
            kv_y_in(step, far).wait_recv()
            a_c(0, step, far).start()

    for index in range(1, z_size):
        step = order[index]
        for kind in (1, 0, 2):
            a_z_in(kind, step).wait_recv()
            a_z_next(kind, index)
            a_x(kind, step).start()
            if kind:
                a_c(kind, step, 0).start()
            else:
                kv_y(step, 0).start()
        if index == z_size - 2:
            d_z_start()
        if index == z_size - 1:
            for copy in own_f:
                copy.wait()

            @pl.when(inner)
            def _():
                for kind in range(3):
                    own_tail(kind).wait()

            for kind in range(3):
                for away, sent in ((1, first_z), (3, last_z), (2, 0)):

                    @pl.when(sent == 0 if away != 2 else me_z >= 0)
                    def _(kind=kind, away=away):
                        f_z(kind, away, lambda copy: copy.start())

            for kind in range(3):
                f_x_start(kind, 0)
                f_c(kind, 0, 0).start()
        if index >= 2:
            from_x(index - 2)
            from_y(index - 2)
    for index in (z_size - 2, z_size - 1):
        from_x(index)
        from_y(index)

    def hand_on(kind, step):
        f_z_wait(kind, step)
        f_x_start(kind, step)
        f_c(kind, step, 0).start()

    def cross(kind, step):
        f_x_wait(kind, step)
        f_c(kind, step, 1).start()

    def pass_cotangent(step):
        d_z_in(order[step]).wait_recv()

        @pl.when(inner)
        def _():
            d_z(step).start()

        d_y(order[step]).start()

    def pass_if(case, step):
        @pl.when(case)
        def _():
            pass_cotangent(step)

    outer = first_z + last_z > 0
    tok_y_in.wait_recv()
    own_q.wait()
    own_o.wait()
    for kind in (0, 1):
        for step in range(z_size):
            for far in range(2):
                a_c_in(kind, step, far).wait_recv()

    gains = kv_w[:, 2 * head :].astype(jnp.float32).T[:8, :]
    gain_ref[...] = gains

    def norm_rows(index, carry):
        at = pl.ds(pl.multiple_of(index * 32, 32), 32)
        values = tok[at, :].astype(jnp.float32)
        scale = lax.rsqrt(jnp.mean(values * values, axis=-1, keepdims=True) + epsilon)
        n1_ref[at, :] = (values * scale * gain_ref[0:1, :]).astype(jnp.bfloat16)
        return carry

    lax.fori_loop(0, 2 * own // 32, norm_rows, 0)
    hand_on(0, order[1])
    table = (table_ref[0], table_ref[1])
    key_ref[...] = spin(dot_nn(n1_ref[...], kv_w[:, :head]), table).astype(jnp.bfloat16)
    val_ref[...] = dot_nn(n1_ref[...], kv_w[:, head : 2 * head]).astype(jnp.bfloat16)
    hand_on(0, order[2])
    head_scale = head ** (-0.5)
    heads = att_ref.shape[1] // head

    half_cols = att_ref.shape[1] // 2
    for index in range(2):
        cols = pl.ds(index * half_cols, half_cols)
        query[:, cols] = dot_nn(n1_ref[...], q_w[:, cols])

    def attend(index):
        cols = pl.ds(index * head, head)
        rotated = (spin(query[:, cols], table) * head_scale).astype(jnp.bfloat16)
        rot_ref[:, cols] = rotated
        probs = head_probs(rotated, key_ref[...], allow_ref[...]).astype(jnp.bfloat16)
        att_ref[:, cols] = dot_nn(probs, val_ref[...]).astype(jnp.bfloat16)

    tasks = [
        lambda: (pass_cotangent(1), pass_if(inner, 2)),
        lambda: hand_on(0, order[3]),
        lambda: (cross(0, 0), hand_on(1, order[1])),
        lambda: cross(1, 0),
        lambda: (cross(2, 0), hand_on(1, order[2])),
    ]
    for index in range(heads):
        attend(index)
        if index < len(tasks):
            tasks[index]()
    for step in range(z_size):
        for far in range(2):
            a_c_in(2, step, far).wait_recv()
    saves = [
        local(kv_w, kv_out),
        local(q_w, wq_out),
        local(o_w, wo_out),
    ]
    span = width // 4

    def project(index, carry):
        cols = pl.ds(pl.multiple_of(index * span, span), span)
        part[:, cols] = matmul_nt(att_ref[...], o_w[cols, :]).astype(jnp.bfloat16)
        return carry

    lax.fori_loop(0, 4, project, 0)
    part_out.start()
    hand_on(1, order[3])
    pass_if(outer, 2)
    pass_if(inner, 3)
    cross(0, order[1])
    hand_on(2, order[1])
    part_out.wait_recv()

    def middle(index, carry):
        at = pl.ds(pl.multiple_of(index * 32, 32), 32)
        there = pl.ds(pl.multiple_of(me_y * own + index * 32, 32), 32)
        values = (
            tok_ref[at, :].astype(jnp.float32)
            + part[there, :].astype(jnp.float32)
            + part_y[at, :].astype(jnp.float32)
        )
        mid_ref[at, :] = values
        scale = lax.rsqrt(jnp.mean(values * values, axis=-1, keepdims=True) + epsilon)
        n2_ref[there, :] = (values * scale * gain_ref[1:2, :]).astype(jnp.bfloat16)
        return carry

    lax.fori_loop(0, own // 32, middle, 0)
    n2_y.start()
    hand_on(2, order[2])
    cross(0, order[2])
    cross(0, order[3])
    hand_on(2, order[3])
    pass_if(outer, 3)
    for kind in (1, 2):
        for index in (1, 2, 3):
            cross(kind, order[index])
    for kind in range(3):
        for step in range(z_size):
            for far in range(2):
                f_c_in(kind, step, far).wait_recv()
    for step in range(z_size):
        d_y_in(step).wait_recv()
    n2_y_in.wait_recv()

    for kind in range(3):
        a_z_done(kind)
    d_z_done()
    tok_y.wait_send()
    part_out.wait_send()
    n2_y.wait_send()
    own_d.wait()
    for copy in saves:
        copy.wait()
    for step in range(z_size):
        d_y(step).wait_send()
        for far in range(2):
            kv_y(step, far).wait_send()
        for kind in range(3):
            if step:
                f_z(kind, step, lambda copy: copy.wait_send())
            a_x(kind, step).wait_send()
            f_x_done(kind, step)
            for far in range(2):
                a_c(kind, step, far).wait_send()
                f_c(kind, step, far).wait_send()


def pre_call(tokens, w_kv, gains, table, segments, cotangent, w_query, w_out, ffn):
    z_size = lax.axis_size("z")
    own, width = tokens.shape
    seq = 2 * own
    rows, cols = w_query.shape
    head = table.shape[2] * 2
    units = ragged_split(ffn[0].shape[1], z_size)[1]
    low = lambda *dims: jax.ShapeDtypeStruct(dims, jnp.bfloat16)
    full = lambda *dims: jax.ShapeDtypeStruct(dims, jnp.float32)
    dma = lambda *lead: pltpu.SemaphoreType.DMA(lead)
    vmem = pl.BlockSpec(memory_space=pltpu.VMEM)
    hbm = pl.BlockSpec(memory_space=pl.ANY)
    wide = lambda *lead: pltpu.VMEM((*lead, width), jnp.bfloat16)
    return pl.pallas_call(
        functools.partial(pre_kernel, z_size),
        out_shape=(
            low(seq, width),
            low(seq, cols),
            low(seq, head),
            low(seq, head),
            low(seq, cols),
            full(own, width),
            low(seq, width),
            full(8, width),
            full(seq, seq),
            low(width, 2 * head + 128),
            low(width, cols),
            low(width, cols),
            low(3, width, units),
            low(z_size, seq, width),
        ),
        in_specs=[vmem] * 5 + [hbm] * 6,
        out_specs=(vmem,) * 9 + (hbm,) * 5,
        scratch_shapes=[
            pltpu.VMEM((width, 2 * head + 128), jnp.bfloat16),
            pltpu.VMEM((width, cols), jnp.bfloat16),
            pltpu.VMEM((width, cols), jnp.bfloat16),
            wide(seq),
            wide(seq),
            wide(own),
            pltpu.VMEM((seq, cols), jnp.float32),
            dma(4),
            dma(4),
            dma(2 * z_size),
            dma(2 * z_size),
            dma(3, z_size + 1),
            dma(3, z_size),
            dma(3, z_size),
            dma(3, z_size),
            dma(3, 2 * z_size),
            dma(3, 2 * z_size),
            dma(3, z_size, 2),
            dma(3, z_size, 2),
            dma(3, z_size),
            dma(3, z_size),
            dma(3, 2 * z_size),
            dma(3, 2 * z_size),
            dma(z_size + 1),
            dma(z_size),
            dma(z_size),
            dma(z_size),
            dma(16),
        ],
        compiler_params=pltpu.CompilerParams(
            collective_id=1, has_side_effects=True, vmem_limit_bytes=VMEM_BYTES
        ),
        cost_estimate=pl.CostEstimate(
            flops=8 * seq * width * cols,
            bytes_accessed=8 * width * (cols + units),
            transcendentals=seq * seq * cols // head,
        ),
    )(tokens, w_kv, gains, table, segments, cotangent, w_query, w_out, *ffn)


def post_kernel(
    z_size,
    main,
    tok_ref,
    gain_ref,
    gain_part_ref,
    n1_ref,
    rot_ref,
    key_ref,
    val_ref,
    att_ref,
    table_ref,
    allow_ref,
    kv_hbm,
    wq_hbm,
    wo_hbm,
    mix_hbm,
    gmf_hbm,
    gmb_hbm,
    mid_hbm,
    sums_hbm,
    mixed_ref,
    tgrad_ref,
    gsum_ref,
    kvg_ref,
    qg_ref,
    og_ref,
    ffn_out,
    kv_w,
    q_w,
    o_w,
    o_part,
    gm,
    gm_f,
    gq,
    gkv,
    kv_sum,
    back_y,
    mix_y,
    mix_z,
    mix_s,
    o_c,
    o_x,
    o_z,
    q_c,
    q_x,
    q_z,
    kv_y,
    kv_c,
    kv_x,
    kv_z,
    gain_own,
    gain_in,
    ffn_in,
    ffn_own,
    load_sem,
    own_sem,
    fx_send,
    fx_recv,
    fz_send,
    fz_recv,
    y_send,
    y_recv,
    my_send,
    my_recv,
    mz_send,
    mz_recv,
    wc_send,
    wc_recv,
    wx_send,
    wx_recv,
    wz_send,
    wz_recv,
    kc_send,
    kc_recv,
    kz_send,
    kz_recv,
    g_send,
    g_recv,
):
    me_z, me_x = lax.axis_index("z"), lax.axis_index("x")
    me_c, me_y = lax.axis_index("c"), lax.axis_index("mp")
    own, width = tok_ref.shape
    seq = 2 * own
    head = key_ref.shape[1]
    cols_here = att_ref.shape[1]
    heads = cols_here // head
    rows = qg_ref.shape[0]
    span = width // z_size
    mine = pl.ds(pl.multiple_of(me_y * own, own), own)
    theirs = pl.ds(pl.multiple_of((1 - me_y) * own, own), own)
    to_y, to_x, to_c = {"mp": 1 - me_y}, {"x": 1 - me_x}, {"c": 1 - me_c}
    head_scale = head ** (-0.5)

    def behind(step):
        return lax.rem(me_z - step + z_size, z_size)

    def to_z(step):
        return {"z": lax.rem(me_z + step, z_size)}

    def row_block(step, x_at, c_at):
        start = ((behind(step) * 2 + x_at) * 2 + c_at) * rows
        return pl.ds(pl.multiple_of(start, rows), rows)

    loads = [
        pltpu.make_async_copy(wo_hbm, o_w, load_sem.at[0]),
        pltpu.make_async_copy(wq_hbm, q_w, load_sem.at[1]),
        pltpu.make_async_copy(
            kv_hbm.at[:, :, :, :, :, pl.ds(0, 2 * head)], kv_w, load_sem.at[2]
        ),
    ]
    for step in range(z_size):
        loads.append(
            pltpu.make_async_copy(mix_hbm.at[step, me_y], mix_s.at[step], load_sem.at[3 + step])
        )
    loads.append(pltpu.make_async_copy(gmf_hbm, gm_f, load_sem.at[3 + z_size]))
    loads.append(pltpu.make_async_copy(gmb_hbm, gm.at[mine], load_sem.at[4 + z_size]))
    mid_load = pltpu.make_async_copy(mid_hbm, gm_f, load_sem.at[5 + z_size])
    for load in loads:
        load.start()

    barrier = pltpu.get_barrier_semaphore()
    peers = [to_y, to_x, to_c] + [to_z(step) for step in range(1, z_size)]
    for where in peers:
        pl.semaphore_signal(barrier, inc=1, device_id=where, device_id_type=MESH_ID)
    pl.semaphore_wait(barrier, len(peers))

    tasks = [(step, kind) for step in (2, 3) for kind in range(3)]

    def f_x(index):
        step, kind = tasks[index]
        return remote(
            sums_hbm.at[kind, step, 1],
            ffn_in.at[index],
            fx_send.at[index],
            fx_recv.at[index],
            to_x,
        )

    def f_own(index):
        step, kind = tasks[index]
        return pltpu.make_async_copy(
            sums_hbm.at[kind, step, 0], ffn_own.at[index % 2], own_sem.at[index % 2]
        )

    def f_z(step, kind, source_z, act):
        for case, columns in (
            ((source_z > 0) & (source_z < z_size - 1), ffn_out.shape[3]),
            ((source_z == 0) | (source_z == z_size - 1), main),
        ):

            @pl.when(case)
            def _(columns=columns):
                cols = pl.ds(0, columns)
                if step == 1:
                    src = sums_hbm.at[kind, 1, 0, :, cols]
                else:
                    src = ffn_in.at[tasks.index((step, kind)), :, cols]
                act(
                    remote(
                        src,
                        ffn_out.at[kind, step, :, cols],
                        fz_send.at[kind, step],
                        fz_recv.at[kind, step],
                        to_z(step),
                    )
                )

    def tick(index):
        step, kind = tasks[index]
        f_x(index).wait_recv()
        f_own(index).wait()
        block = ffn_in.at[index]
        add_rows(block, [ffn_own.at[index % 2]], block, rows)
        if index + 2 < len(tasks):
            f_own(index + 2).start()
        f_z(step, kind, me_z, lambda copy: copy.start())

    def f_x_own(kind):
        return remote(
            sums_hbm.at[kind, 0, 1],
            ffn_out.at[kind, 0],
            fx_send.at[len(tasks) + kind],
            fx_recv.at[len(tasks) + kind],
            to_x,
        )

    f_own(0).start()
    f_own(1).start()
    for index in range(len(tasks)):
        f_x(index).start()
    for kind in range(3):
        f_z(1, kind, me_z, lambda copy: copy.start())

    gm_y = remote(gmb_hbm, gm.at[mine], y_send.at[0], y_recv.at[0], to_y)
    gm_y_in = remote(gm.at[theirs], gm.at[theirs], y_send.at[0], y_recv.at[0], to_y)
    gm_y.start()

    first_z, last_z = (z_size - 1 - me_z) // (z_size - 1), me_z // (z_size - 1)
    inner = first_z + last_z == 0
    order = (
        0,
        1 + (me_z + 1) // 2,
        2 + (2 * me_z - 3) * (1 - first_z - last_z),
        3 - 2 * (me_z // 2),
    )
    right = (None, 1 - me_z // 2, (3 - me_z) * (2 - me_z) // 6 + me_z // 2 * (1 - last_z), 1 - me_z // 2)

    def hop_slot(index):
        step, way = order[index], right[index]
        return way * lax.rem(step + 1, z_size) + (1 - way) * (step - 1 + 4 * ((3 - step) // 2))

    def hop_target(index):
        return {"z": me_z + 2 * right[index] - 1}

    def mix_over_y(step):
        return remote(
            mix_hbm.at[step, 1 - me_y], mix_y.at[step], my_send.at[step], my_recv.at[step], to_y
        )

    def mix_over_z(index):
        slot = hop_slot(index)
        return remote(
            mix_s.at[order[index]],
            mix_z.at[slot],
            mz_send.at[index],
            mz_recv.at[slot],
            hop_target(index),
        )

    def mix_z_in(slot):
        return remote(mix_z.at[slot], mix_z.at[slot], mz_send.at[1], mz_recv.at[slot], to_z(1))

    def mix_add(step, others, last):
        def add_tile(tile, carry):
            at = pl.ds(pl.multiple_of(tile * TILE, TILE), TILE)
            total = mix_s[step, at, :].astype(jnp.float32)
            for other in others:
                total = total + other[at, :].astype(jnp.float32)
            if last:
                mixed_ref[:, at] = (gm_f[:, at] + total.T).astype(jnp.bfloat16)
            else:
                mix_s[step, at, :] = total.astype(jnp.bfloat16)
            return carry

        lax.fori_loop(0, width // TILE, add_tile, 0)

    def mix_step(index):
        step = order[index]
        mix_over_y(step).wait_recv()
        from_y = mix_y.at[step]
        if index:

            @pl.when(inner)
            def _():
                mix_z_in(step).wait_recv()
                mix_add(step, [from_y, mix_z.at[step]], False)

            @pl.when(first_z + last_z > 0)
            def _():
                mix_add(step, [from_y], False)

            mix_over_z(index).start()
        else:
            mid_load.wait()

            @pl.when(first_z == 0)
            def _():
                mix_z_in(0).wait_recv()

            @pl.when(last_z == 0)
            def _():
                mix_z_in(z_size).wait_recv()

            @pl.when(inner)
            def _():
                mix_add(0, [from_y, mix_z.at[0], mix_z.at[z_size]], True)

            @pl.when(first_z > 0)
            def _():
                mix_add(0, [from_y, mix_z.at[z_size]], True)

            @pl.when(last_z > 0)
            def _():
                mix_add(0, [from_y, mix_z.at[0]], True)

    for index in (1, 2, 3, 0):
        mix_over_y(order[index]).start()

    kinds = ((o_part, o_c, o_x, o_z, og_ref), (o_w, q_c, q_x, q_z, qg_ref))

    def w_c(kind, step, far):
        x_at = 1 - me_x if far else me_x
        return remote(
            kinds[kind][0].at[row_block(step, x_at, 1 - me_c)],
            kinds[kind][1].at[step, far],
            wc_send.at[kind, step, far],
            wc_recv.at[kind, step, far],
            to_c,
        )

    def w_x(kind, step):
        return remote(
            kinds[kind][0].at[row_block(step, 1 - me_x, me_c)],
            kinds[kind][2].at[step],
            wx_send.at[kind, step],
            wx_recv.at[kind, step],
            to_x,
        )

    def w_z(kind, index):
        step, slot = order[index], hop_slot(index)
        return remote(
            kinds[kind][0].at[row_block(step, me_x, me_c)],
            kinds[kind][3].at[slot],
            wz_send.at[kind, index],
            wz_recv.at[kind, slot],
            hop_target(index),
        )

    def w_z_in(kind, slot):
        block = kinds[kind][3].at[slot]
        return remote(block, block, wz_send.at[kind, 1], wz_recv.at[kind, slot], to_z(1))

    def w_x_stage(kind, index):
        step = order[index]
        w_c(kind, step, 1).wait_recv()
        block = kinds[kind][0].at[row_block(step, 1 - me_x, me_c)]
        add_rows(block, [kinds[kind][1].at[step, 1]], block, rows)
        w_x(kind, step).start()

    def w_z_stage(kind, index):
        part, from_c, from_x, from_z, result = kinds[kind]
        step = order[index]
        w_c(kind, step, 0).wait_recv()
        w_x(kind, step).wait_recv()
        block = part.at[row_block(step, me_x, me_c)]
        others = [from_c.at[step, 0], from_x.at[step]]
        if index:

            @pl.when(inner)
            def _():
                w_z_in(kind, step).wait_recv()
                add_rows(block, [*others, from_z.at[step]], block, rows)

            @pl.when(first_z + last_z > 0)
            def _():
                add_rows(block, others, block, rows)

            w_z(kind, index).start()
        else:

            @pl.when(first_z == 0)
            def _():
                w_z_in(kind, 0).wait_recv()

            @pl.when(last_z == 0)
            def _():
                w_z_in(kind, z_size).wait_recv()

            @pl.when(inner)
            def _():
                add_rows(block, [*others, from_z.at[0], from_z.at[z_size]], result, rows)

            @pl.when(first_z > 0)
            def _():
                add_rows(block, [*others, from_z.at[z_size]], result, rows)

            @pl.when(last_z > 0)
            def _():
                add_rows(block, [*others, from_z.at[0]], result, rows)

    def w_product(kind, index, left, values):
        step = order[index]
        at = pl.ds(pl.multiple_of(behind(step) * span, 128), span)
        turned = left[:, at].T

        def tile_body(tile, carry):
            cols = pl.ds(pl.multiple_of(tile * TILE, TILE), TILE)
            kinds[kind][0][at, cols] = dot_nn(turned, values[:, cols]).astype(jnp.bfloat16)
            return carry

        lax.fori_loop(0, cols_here // TILE, tile_body, 0)
        for far in (1, 0):
            w_c(kind, step, far).start()

    outer = first_z + last_z > 0

    def if_outer(act, *args):
        @pl.when(outer)
        def _():
            act(*args)

    def if_inner(act, *args):
        @pl.when(inner)
        def _():
            act(*args)

    tick(0)
    tick(1)
    loads[-1].wait()
    gm_y_in.wait_recv()
    w_product(0, 1, gm, att_ref)
    w_product(0, 2, gm, att_ref)
    w_x_stage(0, 1)
    tick(2)
    w_product(0, 3, gm, att_ref)
    w_x_stage(0, 2)
    w_product(0, 0, gm, att_ref)
    w_x_stage(0, 3)
    tick(3)
    for load in loads[:-1]:
        load.wait()
    if_outer(mix_step, 1)

    kv_sum[...] = jnp.zeros(kv_sum.shape, jnp.float32)
    table = (table_ref[0], table_ref[1])

    for index in range(2):
        cols = pl.ds(index * (cols_here // 2), cols_here // 2)
        gq[:, cols] = dot_nn(gm[...], o_w[:, cols]).astype(jnp.bfloat16)

    def attend_back(index):
        cols = pl.ds(index * head, head)
        grad_vals = gq[:, cols]
        rotated = rot_ref[:, cols]
        probs = head_probs(rotated, key_ref[...], allow_ref[...])
        grad_probs = matmul_nt(grad_vals, val_ref[...])
        delta = jnp.sum(probs * grad_probs, axis=-1, keepdims=True)
        grad_scores = (probs * (grad_probs - delta)).astype(jnp.bfloat16)
        grad_rot = dot_nn(grad_scores, key_ref[...])
        gq[:, cols] = (spin_back(grad_rot, table) * head_scale).astype(jnp.bfloat16)
        kv_sum[0] += matmul_tn(grad_scores, rotated)
        kv_sum[1] += matmul_tn(probs.astype(jnp.bfloat16), grad_vals)

    between = {
        0: lambda: (w_x_stage(0, 0), tick(4)),
        1: lambda: (tick(5), if_outer(mix_step, 2)),
        2: lambda: if_inner(mix_step, 1),
        4: lambda: (if_outer(mix_step, 3), if_outer(w_z_stage, 0, 1)),
    }
    for index in range(heads):
        attend_back(index)
        if index in between:
            between[index]()
    gkv[:, :head] = spin_back(kv_sum[0], table).astype(jnp.bfloat16)
    gkv[:, head:] = kv_sum[1].astype(jnp.bfloat16)

    w_product(1, 1, n1_ref, gq)
    w_product(1, 2, n1_ref, gq)
    w_x_stage(1, 1)
    if_inner(mix_step, 2)
    w_product(1, 3, n1_ref, gq)
    w_x_stage(1, 2)
    if_outer(w_z_stage, 0, 2)
    w_product(1, 0, n1_ref, gq)
    w_x_stage(1, 3)
    w_x_stage(1, 0)

    gm_y.wait_send()
    back = gm
    def input_tile(index, carry):
        at = pl.ds(pl.multiple_of(index * span, 128), span)
        back[:, at] = (
            matmul_nt(gq[...], q_w[at, :]) + matmul_nt(gkv[...], kv_w[index].reshape(span, 2 * head))
        ).astype(jnp.bfloat16)
        return carry

    lax.fori_loop(0, z_size, input_tile, 0)
    back_out = remote(back.at[theirs], back_y, y_send.at[1], y_recv.at[1], to_y)
    back_out.start()

    kv_part = kv_w

    def kv_tile(index, carry):
        at = pl.ds(pl.multiple_of(index * span, 128), span)
        product = dot_nn(n1_ref[:, at].T, gkv[...]).astype(jnp.bfloat16)
        kv_part[index] = product.reshape(kv_part.shape[1:])
        return carry

    lax.fori_loop(0, z_size, kv_tile, 0)
    kv_over_y = remote(kv_part.at[:, :, :, 1 - me_y], kv_y, y_send.at[2], y_recv.at[2], to_y)
    kv_over_y.start()
    if_inner(w_z_stage, 0, 1)
    if_outer(w_z_stage, 0, 3)
    if_inner(mix_step, 3)
    if_inner(w_z_stage, 0, 2)
    if_outer(w_z_stage, 1, 1)

    back_out.wait_recv()

    def input_rows(index, total):
        at = pl.ds(pl.multiple_of(index * 32, 32), 32)
        there = pl.ds(pl.multiple_of(me_y * own + index * 32, 32), 32)
        upstream = back[there, :].astype(jnp.float32) + back_y[at, :].astype(jnp.float32)
        grad, gain_part = norm_back(
            tok_ref[at, :].astype(jnp.float32), gain_ref[0:1, :], upstream
        )
        tgrad_ref[at, :] = (gm_f[at, :] + grad).astype(jnp.bfloat16)
        return total + gain_part

    attn_gain_part = lax.fori_loop(
        0, own // 32, input_rows, jnp.zeros((1, width), jnp.float32)
    )
    for index in range(4):
        at = slice(index * span, (index + 1) * span)
        gain_own[0, index : index + 1, :] = attn_gain_part[:, at]
        gain_own[0, 4 + index : 5 + index, :] = gain_part_ref[4 + index : 5 + index, :]

    def gain_send(stage, where):
        return remote(
            gain_own.at[stage], gain_in.at[stage], g_send.at[stage], g_recv.at[stage], where
        )

    gain_hops = [gain_send(0, to_y), gain_send(1, to_c), gain_send(2, to_x)]
    gain_last = [
        remote(
            gain_own.at[3], gain_in.at[2 + step], g_send.at[2 + step], g_recv.at[2 + step], to_z(step)
        )
        for step in range(1, z_size)
    ]

    def gain_fold(stage):
        gain_hops[stage].wait_recv()
        gain_own[stage + 1] = gain_own[stage] + gain_in[stage]

    gain_hops[0].start()
    mid_load.start()
    if_inner(w_z_stage, 0, 3)
    if_outer(w_z_stage, 1, 2)
    if_inner(w_z_stage, 1, 1)
    gain_fold(0)
    gain_hops[1].start()
    if_outer(w_z_stage, 1, 3)
    mix_step(0)
    if_inner(w_z_stage, 1, 2)
    gain_fold(1)
    gain_hops[2].start()
    w_z_stage(0, 0)
    kv_over_y.wait_recv()

    def kv_add_y(index, carry):
        for x_at in range(2):
            for c_at in range(2):
                block = kv_part.at[index, x_at, c_at, me_y]
                block[...] = (
                    block[...].astype(jnp.float32) + kv_y[index, x_at, c_at].astype(jnp.float32)
                ).astype(jnp.bfloat16)
        return carry

    lax.fori_loop(0, z_size, kv_add_y, 0)
    kv_over_c = remote(
        kv_part.at[:, :, 1 - me_c, me_y], kv_c, kc_send.at[0], kc_recv.at[0], to_c
    )
    kv_over_c.start()
    gain_fold(2)
    for copy in gain_last:
        copy.start()
    kv_over_c.wait_recv()

    def kv_add_c(index, carry):
        for x_at in range(2):
            block = kv_part.at[index, x_at, me_c, me_y]
            block[...] = (
                block[...].astype(jnp.float32) + kv_c[index, x_at].astype(jnp.float32)
            ).astype(jnp.bfloat16)
        return carry

    lax.fori_loop(0, z_size, kv_add_c, 0)
    kv_over_x = remote(
        kv_part.at[:, 1 - me_x, me_c, me_y], kv_x, kc_send.at[1], kc_recv.at[1], to_x
    )
    kv_over_x.start()
    for kind in range(3):
        f_x_own(kind).start()
    if_inner(w_z_stage, 1, 3)
    kv_over_x.wait_recv()

    def kv_add_x(index, carry):
        block = kv_part.at[index, me_x, me_c, me_y]
        block[...] = (
            block[...].astype(jnp.float32) + kv_x[index].astype(jnp.float32)
        ).astype(jnp.bfloat16)
        return carry

    lax.fori_loop(0, z_size, kv_add_x, 0)
    kv_over_z = [
        remote(
            kv_part.at[lax.rem(me_z + step, z_size), me_x, me_c, me_y],
            kv_z.at[step - 1],
            kz_send.at[step],
            kz_recv.at[step],
            to_z(step),
        )
        for step in range(1, z_size)
    ]
    for copy in kv_over_z:
        copy.start()
    w_z_stage(1, 0)
    for copy in gain_last:
        copy.wait_recv()
    gsum_ref[...] = gain_own[3] + gain_in[3] + gain_in[4] + gain_in[5]
    for copy in kv_over_z:
        copy.wait_recv()
    kvg_ref[...] = (
        kv_part[me_z, me_x, me_c, me_y].astype(jnp.float32)
        + kv_z[0].astype(jnp.float32)
        + kv_z[1].astype(jnp.float32)
        + kv_z[2].astype(jnp.float32)
    )

    back_out.wait_send()
    kv_over_y.wait_send()
    kv_over_c.wait_send()
    kv_over_x.wait_send()
    for kind in range(3):
        f_x_own(kind).wait()
    for index in range(len(tasks)):
        f_x(index).wait_send()
    for step in range(1, z_size):
        for kind in range(3):
            f_z(step, kind, me_z, lambda copy: copy.wait_send())
            f_z(step, kind, behind(step), lambda copy: copy.wait_recv())
    for copy in gain_hops + gain_last + kv_over_z:
        copy.wait_send()
    for step in range(z_size):
        mix_over_y(step).wait_send()
        if step:
            mix_over_z(step).wait_send()
        for kind in range(2):
            w_c(kind, step, 0).wait_send()
            w_c(kind, step, 1).wait_send()
            w_x(kind, step).wait_send()
            if step:
                w_z(kind, step).wait_send()


def post_call(
    tokens,
    gains,
    gain_part,
    normed_one,
    rotated,
    keys,
    values,
    attn_vals,
    table,
    allowed,
    kv_weight,
    query_weight,
    out_weight,
    mix_parts,
    grad_mid,
    grad_mid_low,
    mid,
    ffn_sums,
    main,
):
    z_size = lax.axis_size("z")
    own, width = tokens.shape
    seq = 2 * own
    head = keys.shape[1]
    cols = attn_vals.shape[1]
    rows = width // (4 * z_size)
    units = ffn_sums.shape[4]
    low = lambda *dims: pltpu.VMEM(dims, jnp.bfloat16)
    full = lambda *dims: pltpu.VMEM(dims, jnp.float32)
    out_full = lambda *dims: jax.ShapeDtypeStruct(dims, jnp.float32)
    out_low = lambda *dims: jax.ShapeDtypeStruct(dims, jnp.bfloat16)
    dma = lambda *lead: pltpu.SemaphoreType.DMA(lead)
    vmem = pl.BlockSpec(memory_space=pltpu.VMEM)
    hbm = pl.BlockSpec(memory_space=pl.ANY)
    z = z_size
    return pl.pallas_call(
        functools.partial(post_kernel, z_size, main),
        out_shape=(
            out_low(own, width),
            out_low(own, width),
            out_full(8, width // z),
            out_full(rows // 2, 2 * head),
            out_full(rows, cols),
            out_full(rows, cols),
            out_low(3, z, rows, units),
        ),
        in_specs=[vmem] * 10 + [hbm] * 8,
        out_specs=(vmem,) * 6 + (hbm,),
        scratch_shapes=[
            low(z, 2, 2, 2, rows // 2, 2 * head),
            low(width, cols),
            low(width, cols),
            low(width, cols),
            low(seq, width),
            full(own, width),
            low(seq, cols),
            low(seq, 2 * head),
            full(2, seq, head),
            low(own, width),
            low(z, width, own),
            low(z + 1, width, own),
            low(z, width, own),
            low(z, 2, rows, cols),
            low(z, rows, cols),
            low(z + 1, rows, cols),
            low(z, 2, rows, cols),
            low(z, rows, cols),
            low(z + 1, rows, cols),
            low(z, 2, 2, rows // 2, 2 * head),
            low(z, 2, rows // 2, 2 * head),
            low(z, rows // 2, 2 * head),
            low(z - 1, rows // 2, 2 * head),
            full(4, 8, width // z),
            full(6, 8, width // z),
            low(6, rows, units),
            low(2, rows, units),
            dma(6 + z),
            dma(2),
            dma(9),
            dma(9),
            dma(3, z),
            dma(3, z),
            dma(3),
            dma(3),
            dma(z),
            dma(z),
            dma(z),
            dma(z + 1),
            dma(2, z, 2),
            dma(2, z, 2),
            dma(2, z),
            dma(2, z),
            dma(2, z),
            dma(2, z + 1),
            dma(2),
            dma(2),
            dma(z),
            dma(z),
            dma(6),
            dma(6),
        ],
        compiler_params=pltpu.CompilerParams(
            collective_id=2, has_side_effects=True, vmem_limit_bytes=VMEM_BYTES
        ),
        cost_estimate=pl.CostEstimate(
            flops=14 * seq * width * cols,
            bytes_accessed=10 * width * cols,
            transcendentals=seq * seq * cols // head,
        ),
    )(
        tokens,
        gains,
        gain_part,
        normed_one,
        rotated,
        keys,
        values,
        attn_vals,
        table,
        allowed,
        kv_weight.reshape(z, 2, 2, 2, rows // 2, kv_weight.shape[1]),
        query_weight,
        out_weight,
        mix_parts,
        grad_mid,
        grad_mid_low,
        mid,
        ffn_sums,
    )


def layout_kernel(
    z_size,
    main,
    sum_ref,
    ffn_ref,
    q_ref,
    o_ref,
    kv_ref,
    mixed_in,
    tgrad_in,
    wg_ref,
    wu_ref,
    wd_ref,
    qg_ref,
    og_ref,
    kvg_ref,
    mixed_ref,
    tgrad_ref,
):
    me_z = lax.axis_index("z")
    for kind, out in enumerate((wg_ref, wu_ref, wd_ref)):
        for step in range(z_size):
            at = lax.rem(me_z - step + z_size, z_size)
            values = ffn_ref[kind, step].astype(jnp.float32)
            if step == 0:
                values = values + sum_ref[kind, 0, 0].astype(jnp.float32)
            body = pl.ds(pl.multiple_of(at * main, 128), main)
            out[:, body] = values[:, :main]

            @pl.when((at > 0) & (at < z_size - 1))
            def _(out=out, at=at, values=values):
                tail = z_size * main + lax.rem(at + 1, 2) * 128
                out[:, pl.ds(pl.multiple_of(tail, 128), 128)] = values[:, main:]
    qg_ref[...] = q_ref[...]
    og_ref[...] = o_ref[...]
    kvg_ref[...] = kv_ref[...]
    mixed_ref[...] = mixed_in[...]
    tgrad_ref[...] = tgrad_in[...]


def layout_call(ffn_sums, ffn_grads, query_grad, out_grad, kv_grad, mixed, tokens_grad, ffn_cols):
    z_size = lax.axis_size("z")
    main, units = ragged_split(ffn_cols, z_size)
    rows, cols = query_grad.shape
    parts = rows // 32
    kv_rows = kv_grad.shape[0] // parts
    full = lambda *dims: jax.ShapeDtypeStruct(dims, jnp.float32)
    row = lambda height, width: pl.BlockSpec((height, width), lambda index: (index, 0))
    own, width = mixed.shape
    share = pl.BlockSpec((own, width // parts), lambda index: (0, index))
    specs = [row(32, cols), row(32, cols), row(kv_rows, kv_grad.shape[1]), share, share]
    return pl.pallas_call(
        functools.partial(layout_kernel, z_size, main),
        grid=(parts,),
        out_shape=(
            *[full(rows, ffn_cols)] * 3,
            full(rows, cols),
            full(rows, cols),
            full(*kv_grad.shape),
            jax.ShapeDtypeStruct(mixed.shape, jnp.bfloat16),
            jax.ShapeDtypeStruct(mixed.shape, jnp.bfloat16),
        ),
        in_specs=[
            pl.BlockSpec((3, 1, 1, 32, units), lambda index: (0, 0, 0, index, 0)),
            pl.BlockSpec((3, z_size, 32, units), lambda index: (0, 0, index, 0)),
            *specs,
        ],
        out_specs=(*[row(32, ffn_cols)] * 3, *specs),
        compiler_params=pltpu.CompilerParams(vmem_limit_bytes=VMEM_BYTES),
    )(ffn_sums, ffn_grads, query_grad, out_grad, kv_grad, mixed, tokens_grad)


FF_SPLIT = 4


def ffn_pass(normed, grad_out, gate_weight, up_weight, down_weight):
    gate = jnp.dot(normed, gate_weight, preferred_element_type=jnp.float32)
    up_proj = jnp.dot(normed, up_weight, preferred_element_type=jnp.float32)
    grad_hidden = jnp.dot(grad_out, down_weight, preferred_element_type=jnp.float32)
    product, pull = jax.vjp(gelu_product, gate, up_proj)
    hidden = product.astype(jnp.bfloat16)
    grad_gate_f, grad_up_f = pull(grad_hidden)
    grad_gate = grad_gate_f.astype(jnp.bfloat16)
    grad_up = grad_up_f.astype(jnp.bfloat16)
    mixed_part = matmul_nt(hidden, down_weight).astype(jnp.bfloat16)
    normed_part = (matmul_nt(grad_gate, gate_weight) + matmul_nt(grad_up, up_weight)).astype(
        jnp.bfloat16
    )
    weight_parts = [
        matmul_tn(normed, grad_gate).astype(jnp.bfloat16),
        matmul_tn(normed, grad_up).astype(jnp.bfloat16),
        matmul_tn(grad_out, hidden).astype(jnp.bfloat16),
    ]
    return mixed_part, normed_part, weight_parts


def shards_general(
    tokens,
    segments,
    positions,
    cotangent,
    attn_gain,
    ffn_gain,
    w_kv,
    w_query,
    w_out,
    w_gate,
    w_up,
    w_down,
):
    everywhere = ("z", "xc", "mp")
    dp = ("z", "xc")
    z_size = lax.axis_size("z")
    xc_size = lax.axis_size("xc")
    gains = lax.all_gather(
        jnp.stack([attn_gain, ffn_gain], axis=1), everywhere, axis=0, tiled=True
    ).astype(jnp.float32)
    gain_one, gain_two = gains[:, 0], gains[:, 1]
    kv_weight = lax.all_gather(w_kv, everywhere, axis=0, tiled=True)
    head_dim = kv_weight.shape[1] // 2
    width = tokens.shape[1]
    seq_len = segments.shape[0]
    heads_here = w_query.shape[1] // head_dim
    scale = head_dim ** (-0.5)
    cosine, sine = rotary_angles(positions, head_dim)
    inputs_f = tokens.astype(jnp.float32)
    tokens_all = lax.all_gather(tokens, "mp", axis=0, tiled=True)
    normed_one = norm_gain(tokens_all.astype(jnp.float32), gain_one).astype(jnp.bfloat16)
    query_weight = lax.all_gather(w_query, dp, axis=0, tiled=True)
    out_weight = lax.all_gather(w_out, dp, axis=0, tiled=True)

    rows = w_gate.shape[0]
    unit = w_gate.shape[1] // z_size

    def spread(weight):
        pieces = weight.reshape(rows, z_size, unit).transpose(1, 0, 2)
        pieces = lax.all_to_all(pieces, "z", split_axis=0, concat_axis=0, tiled=True)
        return lax.all_gather(pieces, "xc", axis=1, tiled=False).reshape(width, unit)

    gate_weight, up_weight, down_weight = spread(w_gate), spread(w_up), spread(w_down)
    grad_all = lax.all_gather(cotangent, ("z", "mp"), axis=0, tiled=True)

    query = jnp.dot(normed_one, query_weight, preferred_element_type=jnp.float32).reshape(
        seq_len, heads_here, head_dim
    )
    rotated = (rotate(query, cosine[:, None], sine[:, None]) * scale).astype(jnp.bfloat16)
    keyval = jnp.dot(normed_one, kv_weight, preferred_element_type=jnp.float32)
    keys = rotate(keyval[:, :head_dim], cosine, sine).astype(jnp.bfloat16)
    values = keyval[:, head_dim:].astype(jnp.bfloat16)
    allowed = block_allowed(segments, 0, seq_len)
    scores = jnp.einsum("thd,sd->hts", rotated, keys, preferred_element_type=jnp.float32)
    scores = jnp.where(allowed[None], scores, masked_score)
    row_max = jnp.max(scores, axis=-1, keepdims=True)
    weights = jnp.exp(scores - row_max)
    probs = weights / jnp.sum(weights, axis=-1, keepdims=True)
    probs_low = probs.astype(jnp.bfloat16)
    attn_vals = (
        jnp.einsum("hts,sd->thd", probs_low, values, preferred_element_type=jnp.float32)
        .reshape(seq_len, heads_here * head_dim)
        .astype(jnp.bfloat16)
    )
    mid = inputs_f + lax.psum_scatter(
        matmul_nt(attn_vals, out_weight).astype(jnp.bfloat16),
        "mp",
        scatter_dimension=0,
        tiled=True,
    ).astype(jnp.float32)
    normed_two = norm_gain(mid, gain_two).astype(jnp.bfloat16)
    normed_all = lax.all_gather(normed_two, ("z", "mp"), axis=0, tiled=True)

    mixed_part, normed_part, weight_parts = ffn_pass(
        normed_all, grad_all, gate_weight, up_weight, down_weight
    )
    grad_normed_two = lax.psum_scatter(
        normed_part, ("z", "mp"), scatter_dimension=0, tiled=True
    ).astype(jnp.float32)
    mixed = (
        mid
        + lax.psum_scatter(mixed_part, ("z", "mp"), scatter_dimension=0, tiled=True).astype(
            jnp.float32
        )
    ).astype(jnp.bfloat16)

    def collect(part):
        pieces = part.reshape(z_size, xc_size, rows, unit).transpose(1, 0, 2, 3)
        pieces = pieces.reshape(xc_size * z_size * rows, unit)
        pieces = lax.psum_scatter(pieces, "xc", scatter_dimension=0, tiled=True)
        pieces = pieces.reshape(z_size, rows, unit)
        pieces = lax.all_to_all(pieces, "z", split_axis=0, concat_axis=0, tiled=True)
        return pieces.transpose(1, 0, 2).reshape(rows, z_size * unit).astype(jnp.float32)

    w_gate_grad, w_up_grad, w_down_grad = [collect(part) for part in weight_parts]

    norm_pull_two = jax.vjp(norm_gain, mid, gain_two)[1]
    grad_mid_norm, grad_gain_two = norm_pull_two(grad_normed_two)
    grad_mid = cotangent.astype(jnp.float32) + grad_mid_norm
    grad_mid_all = lax.all_gather(grad_mid.astype(jnp.bfloat16), "mp", axis=0, tiled=True)
    grad_vals = (
        jnp.dot(grad_mid_all, out_weight, preferred_element_type=jnp.float32)
        .astype(jnp.bfloat16)
        .reshape(seq_len, heads_here, head_dim)
    )
    grad_probs = jnp.einsum("thd,sd->hts", grad_vals, values, preferred_element_type=jnp.float32)
    delta = jnp.sum(probs * grad_probs, axis=-1, keepdims=True)
    grad_scores = (probs * (grad_probs - delta)).astype(jnp.bfloat16)
    grad_rot = jnp.einsum("hts,sd->thd", grad_scores, keys, preferred_element_type=jnp.float32)
    key_sum = jnp.einsum("hts,thd->sd", grad_scores, rotated, preferred_element_type=jnp.float32)
    value_sum = jnp.einsum("hts,thd->sd", probs_low, grad_vals, preferred_element_type=jnp.float32)
    grad_query = (
        (unrotate(grad_rot, cosine[:, None], sine[:, None]) * scale)
        .reshape(seq_len, heads_here * head_dim)
        .astype(jnp.bfloat16)
    )
    grad_kv = jnp.concatenate([unrotate(key_sum, cosine, sine), value_sum], axis=1).astype(
        jnp.bfloat16
    )
    grad_normed_one = lax.psum_scatter(
        (matmul_nt(grad_query, query_weight) + matmul_nt(grad_kv, kv_weight)).astype(jnp.bfloat16),
        "mp",
        scatter_dimension=0,
        tiled=True,
    ).astype(jnp.float32)
    norm_pull_one = jax.vjp(norm_gain, inputs_f, gain_one)[1]
    grad_input_norm, grad_gain_one = norm_pull_one(grad_normed_one)
    tokens_grad = (grad_mid + grad_input_norm).astype(jnp.bfloat16)

    w_query_grad = lax.psum_scatter(
        matmul_tn(normed_one, grad_query).astype(jnp.bfloat16), dp, scatter_dimension=0, tiled=True
    ).astype(jnp.float32)
    w_out_grad = lax.psum_scatter(
        matmul_tn(grad_mid_all, attn_vals).astype(jnp.bfloat16), dp, scatter_dimension=0, tiled=True
    ).astype(jnp.float32)
    small = jnp.concatenate(
        [matmul_tn(normed_one, grad_kv), grad_gain_one[:, None], grad_gain_two[:, None]], axis=1
    )
    small = lax.psum_scatter(small, everywhere, scatter_dimension=0, tiled=True)
    kv_grad = small[:, : 2 * head_dim]
    return (
        mixed,
        tokens_grad,
        small[:, 2 * head_dim],
        small[:, 2 * head_dim + 1],
        kv_grad,
        w_query_grad,
        w_out_grad,
        w_gate_grad,
        w_up_grad,
        w_down_grad,
    )


def shards_fast(
    tokens,
    segments,
    positions,
    cotangent,
    attn_gain,
    ffn_gain,
    w_kv,
    w_query,
    w_out,
    w_gate,
    w_up,
    w_down,
):
    seq_len = segments.shape[0]
    cosine, sine = rotary_angles(positions, w_kv.shape[1] // 2)
    table = jnp.stack(
        [
            jnp.concatenate([cosine, cosine], axis=1),
            jnp.concatenate([-sine, sine], axis=1),
        ]
    )
    gain_rows = jnp.pad(
        jnp.stack([attn_gain, ffn_gain]).astype(jnp.float32),
        ((0, 6), (0, 128 - attn_gain.shape[0])),
    )
    segment_rows = jnp.broadcast_to(segments.astype(jnp.float32)[None, :], (8, seq_len))
    (
        normed_one,
        rotated,
        keys,
        values,
        attn_vals,
        mid,
        normed_two,
        gains,
        allowed,
        kv_weight,
        query_weight,
        out_weight,
        ffn_weights,
        grad_all,
    ) = pre_call(
        tokens,
        w_kv,
        gain_rows,
        table,
        segment_rows,
        cotangent,
        w_query,
        w_out,
        (w_gate, w_up, w_down),
    )
    main = ragged_split(w_gate.shape[1], lax.axis_size("z"))[0]
    grad_mid, gain_part, mix_parts, ffn_sums, grad_mid_low = ffn_call(
        gains, normed_two, grad_all, ffn_weights, mid, w_gate.shape[0], main
    )
    mixed, tokens_grad, gain_grads, kv_grad, query_grad, out_grad, ffn_grads = post_call(
        tokens,
        gains,
        gain_part,
        normed_one,
        rotated,
        keys,
        values,
        attn_vals,
        table,
        allowed,
        kv_weight,
        query_weight,
        out_weight,
        mix_parts,
        grad_mid,
        grad_mid_low,
        mid,
        ffn_sums,
        main,
    )
    *ffn_out, query_grad, out_grad, kv_grad, mixed, tokens_grad = layout_call(
        ffn_sums,
        ffn_grads,
        query_grad,
        out_grad,
        kv_grad,
        mixed,
        tokens_grad,
        w_gate.shape[1],
    )
    share = attn_gain.shape[0]
    place = lax.axis_index(("z", "x", "c", "mp")) * share
    gain_grads = gain_grads.reshape(2, gain_grads.size // 2)
    gain_grads = lax.dynamic_slice(gain_grads, (0, place), (2, share))
    return (
        mixed,
        tokens_grad,
        gain_grads[0],
        gain_grads[1],
        kv_grad,
        query_grad,
        out_grad,
        *ffn_out,
    )


def solution(mesh):
    dp_size, mp_size = mesh.shape["dp"], mesh.shape["mp"]
    if dp_size == 4 * FF_SPLIT and mp_size == 2:
        body, dp = shards_fast, ("z", "x", "c")
        sizes = (FF_SPLIT, 2, 2, mp_size)
    else:
        body, dp = shards_general, ("z", "xc")
        sizes = (FF_SPLIT, dp_size // FF_SPLIT, mp_size)
    all_axes = (*dp, "mp")
    fine = jax.sharding.Mesh(mesh.devices.reshape(sizes), all_axes)
    in_specs = (
        P(all_axes, None),
        P(dp),
        P(dp),
        P(all_axes, None),
        P(all_axes),
        P(all_axes),
        P(all_axes, None),
        P(dp, "mp"),
        P(dp, "mp"),
        P(dp, "mp"),
        P(dp, "mp"),
        P(dp, "mp"),
    )
    out_specs = (
        P(all_axes, None),
        P(all_axes, None),
        P(all_axes),
        P(all_axes),
        P(all_axes, None),
        P(dp, "mp"),
        P(dp, "mp"),
        P(dp, "mp"),
        P(dp, "mp"),
        P(dp, "mp"),
    )
    return jax.shard_map(body, mesh=fine, in_specs=in_specs, out_specs=out_specs, check_vma=False)
```

```python
import functools

import jax
import jax.numpy as jnp
from jax import lax
from jax.experimental import pallas as pl
from jax.experimental.pallas import tpu as pltpu
from jax.sharding import PartitionSpec as P

WINDOW = 2048


epsilon = 1e-06
rope_base = 10000.0
masked_score = -1e30
VMEM_BYTES = 66_000_000


def norm_gain(values, gain):
    return values * lax.rsqrt(jnp.mean(values * values, axis=-1, keepdims=True) + epsilon) * gain


def rotary_angles(positions, head_width):
    quarter = head_width // 4
    freqs = rope_base ** (-jnp.arange(quarter).astype(jnp.float32) / quarter)
    phase = positions.astype(jnp.float32)[:, None] * freqs[None, :]
    return (jnp.cos(phase), jnp.sin(phase))


def rotate(values, cosine, sine):
    quarter = cosine.shape[-1]
    first_half = values[..., :quarter]
    second_half = values[..., quarter : 2 * quarter]
    return jnp.concatenate(
        [
            first_half * cosine - second_half * sine,
            second_half * cosine + first_half * sine,
            values[..., 2 * quarter :],
        ],
        axis=-1,
    )


def unrotate(values, cosine, sine):
    quarter = cosine.shape[-1]
    first_half = values[..., :quarter]
    second_half = values[..., quarter : 2 * quarter]
    return jnp.concatenate(
        [
            first_half * cosine + second_half * sine,
            second_half * cosine - first_half * sine,
            values[..., 2 * quarter :],
        ],
        axis=-1,
    )


def gelu_product(gate, up_proj):
    return jax.nn.gelu(gate, approximate=True) * up_proj


def matmul_nt(left, right):
    return lax.dot_general(
        left, right, (((1,), (1,)), ((), ())), preferred_element_type=jnp.float32
    )


def matmul_tn(left, right):
    return lax.dot_general(
        left, right, (((0,), (0,)), ((), ())), preferred_element_type=jnp.float32
    )


def block_allowed(segments, first_row, rows):
    seq_len = segments.shape[0]
    query_rows = first_row + jnp.arange(rows)
    key_rows = jnp.arange(seq_len)
    return (
        (segments[:, None] == segments[None, :])
        & (key_rows[None, :] <= query_rows[:, None])
        & (query_rows[:, None] - key_rows[None, :] < WINDOW)
    )


MESH_ID = pl.DeviceIdType.MESH
GELU_A = 0.7978845608028654
GELU_B = 0.044715
TILE = 256
WIDE = 512


def remote(src, dst, send_sem, recv_sem, where):
    return pltpu.make_async_remote_copy(
        src_ref=src,
        dst_ref=dst,
        send_sem=send_sem,
        recv_sem=recv_sem,
        device_id=where,
        device_id_type=MESH_ID,
    )


def dot_nn(left, right):
    return lax.dot_general(
        left, right, (((1,), (0,)), ((), ())), preferred_element_type=jnp.float32
    )


def gelu_parts(gate):
    square = gate * gate
    bend = jnp.tanh(GELU_A * gate * (1.0 + GELU_B * square))
    half = 0.5 * (1.0 + bend)
    slope = half + 0.5 * gate * (1.0 - bend * bend) * GELU_A * (1.0 + 3.0 * GELU_B * square)
    return gate * half, slope


def add_rows(first, rest, out, count):
    def body(index, carry):
        step = pl.ds(pl.multiple_of(index * 32, 32), 32)
        total = first[step, :].astype(jnp.float32)
        for other in rest:
            total = total + other[step, :].astype(jnp.float32)
        out[step, :] = total.astype(out.dtype)
        return carry

    lax.fori_loop(0, count // 32, body, 0)


def norm_back(values, gain, upstream):
    scale = lax.rsqrt(jnp.mean(values * values, axis=-1, keepdims=True) + epsilon)
    normed = values * scale
    pulled = gain * upstream
    back = scale * (pulled - normed * jnp.mean(normed * pulled, axis=-1, keepdims=True))
    return back, jnp.sum(upstream * normed, axis=0, keepdims=True)


def ffn_kernel(
    z_size,
    main,
    gain_ref,
    own_hbm,
    dy_hbm,
    w_hbm,
    mid_hbm,
    gm_ref,
    gain_part,
    mix_hbm,
    sums_hbm,
    gm_hbm,
    n2,
    dy,
    w3,
    h3,
    n2_t,
    dy_t,
    gn_part,
    mix_buf,
    gn_y,
    gn_z,
    gn_s,
    c_in,
    x_in,
    mid,
    load_sem,
    mix_sem,
    ag_y_send,
    ag_y_recv,
    ag_z_send,
    ag_z_recv,
    rs_y_send,
    rs_y_recv,
    rs_z_send,
    rs_z_recv,
    c_send,
    c_recv,
    x_send,
    x_recv,
    out_sem,
):
    own = own_hbm.shape[0] // 2
    width = own_hbm.shape[1]
    units = w3.shape[2]
    rows = c_in.shape[3]
    span = width // z_size
    me_y, me_z = lax.axis_index("mp"), lax.axis_index("z")
    me_x, me_c = lax.axis_index("x"), lax.axis_index("c")
    mine = pl.ds(pl.multiple_of(me_y * own, own), own)
    theirs = pl.ds(pl.multiple_of((1 - me_y) * own, own), own)
    to_y, to_x, to_c = {"mp": 1 - me_y}, {"x": 1 - me_x}, {"c": 1 - me_c}

    def ahead(step):
        return lax.rem(me_z + step, z_size)

    def to_z(step):
        return {"z": ahead(step)}

    def row_block(z_at, x_at, c_at):
        return pl.ds(pl.multiple_of(((z_at * 2 + x_at) * 2 + c_at) * rows, rows), rows)

    inner = (me_z > 0) & (me_z < z_size - 1)
    outer = (me_z == 0) | (me_z == z_size - 1)

    def w_load(index, columns):
        cols = pl.ds(0, columns)
        return pltpu.make_async_copy(
            w_hbm.at[index, :, cols], w3.at[index, :, cols], load_sem.at[z_size + index]
        )

    def w_loads(act):
        for case, columns in ((inner, units), (outer, main)):

            @pl.when(case)
            def _(columns=columns):
                for index in range(3):
                    act(w_load(index, columns))

    w_loads(lambda copy: copy.start())
    dy_loads = [
        pltpu.make_async_copy(dy_hbm.at[index], dy, load_sem.at[index])
        for index in range(z_size)
    ]
    own_load = pltpu.make_async_copy(own_hbm, n2.at[0], load_sem.at[z_size + 3])
    mid_load = pltpu.make_async_copy(mid_hbm, mid, load_sem.at[z_size + 4])
    for load in (own_load, dy_loads[0], mid_load):
        load.start()

    barrier = pltpu.get_barrier_semaphore()
    peers = [to_y, to_x, to_c] + [to_z(step) for step in range(1, z_size)]
    for where in peers:
        pl.semaphore_signal(barrier, inc=1, device_id=where, device_id_type=MESH_ID)
    pl.semaphore_wait(barrier, len(peers))

    def ag_y(index):
        block = n2.at[index, mine]
        return remote(block, block, ag_y_send.at[index], ag_y_recv.at[index], to_y)

    def ag_y_in(index):
        block = n2.at[index, theirs]
        return remote(block, block, ag_y_send.at[index], ag_y_recv.at[index], to_y)

    def ag_z(index):
        src = own_hbm.at[mine] if index == 0 else n2.at[index, mine]
        return remote(
            src, n2.at[index + 1, mine], ag_z_send.at[index], ag_z_recv.at[index + 1], to_z(1)
        )

    def ag_z_in(index):
        block = n2.at[index, mine]
        return remote(block, block, ag_z_send.at[0], ag_z_recv.at[index], to_z(1))

    def ag_last():
        return remote(
            n2.at[2, theirs], n2.at[3, theirs], ag_y_send.at[3], ag_y_recv.at[3], to_z(1)
        )

    def forward(index):
        ag_z_in(index).wait_recv()
        ag_z(index).start()
        ag_y(index).start()

    ag_z(0).start()

    mix_copies = []

    def turn(source, target, index):
        def turn_tile(tile, carry):
            at = pl.ds(pl.multiple_of(tile * span, 128), span)
            target[at, pl.ds(index * 2 * own, 2 * own)] = source[:, at].T
            return carry

        lax.fori_loop(0, z_size, turn_tile, 0)

    def chunk(index):
        if index:
            mix_copies[index - 1].wait()
        dy_loads[index].wait()
        rows_at = pl.ds(index * 2 * own, 2 * own)

        def up_tile(tile, carry):
            cols = pl.ds(pl.multiple_of(tile * TILE, TILE), TILE)
            gate = dot_nn(n2[index], w3[0, :, cols])
            up_proj = dot_nn(n2[index], w3[1, :, cols])
            grad_hidden = dot_nn(dy[...], w3[2, :, cols])
            act, slope = gelu_parts(gate)
            h3[0, rows_at, cols] = (grad_hidden * up_proj * slope).astype(jnp.bfloat16)
            h3[1, rows_at, cols] = (grad_hidden * act).astype(jnp.bfloat16)
            h3[2, rows_at, cols] = (act * up_proj).astype(jnp.bfloat16)
            return carry

        lax.fori_loop(0, units // TILE, up_tile, 0)

        def down_tile(tile, carry):
            at = pl.ds(pl.multiple_of(tile * span, 128), span)
            normed = matmul_nt(w3[0, at, :], h3[0, rows_at, :]) + matmul_nt(
                w3[1, at, :], h3[1, rows_at, :]
            )
            mixed = matmul_nt(w3[2, at, :], h3[2, rows_at, :])
            for half in range(2):
                cols = slice(half * own, (half + 1) * own)
                gn_part[index, half, at, :] = normed[:, cols].astype(jnp.bfloat16)
                mix_buf[half, at, :] = mixed[:, cols].astype(jnp.bfloat16)
            return carry

        lax.fori_loop(0, z_size, down_tile, 0)
        copy = pltpu.make_async_copy(mix_buf, mix_hbm.at[index], mix_sem.at[index])
        copy.start()
        mix_copies.append(copy)
        if index:
            rs_y(index).start()
        turn(n2.at[index], n2_t, index)
        turn(dy, dy_t, index)
        if index + 1 < z_size:
            dy_loads[index + 1].start()

    def rs_y(index):
        return remote(
            gn_part.at[index, 1 - me_y], gn_y.at[index], rs_y_send.at[index], rs_y_recv.at[index], to_y
        )

    def rs_z(index):
        return remote(
            gn_s.at[index - 1],
            gn_z.at[index - 1],
            rs_z_send.at[index],
            rs_z_recv.at[index - 1],
            to_z(1),
        )

    def rs_step(index):
        rs_y(index).wait_recv()
        slot = (index - 2) % z_size
        if index != 1:
            remote(
                gn_s.at[slot], gn_z.at[slot], rs_z_send.at[1], rs_z_recv.at[slot], to_z(1)
            ).wait_recv()

        def add_tile(tile, carry):
            at = pl.ds(pl.multiple_of(tile * TILE, TILE), TILE)
            total = gn_part[index, me_y, at, :].astype(jnp.float32) + gn_y[index, at, :].astype(
                jnp.float32
            )
            if index != 1:
                total = total + gn_z[slot, at, :].astype(jnp.float32)
            if index == 0:
                gm_ref[:, at] = total.T
            else:
                gn_s[index - 1, at, :] = total.astype(jnp.bfloat16)
            return carry

        lax.fori_loop(0, width // TILE, add_tile, 0)
        if index != 0:
            rs_z(index).start()


    def grads(step):
        at = pl.ds(pl.multiple_of(ahead(step) * span, 128), span)
        for kind, source in enumerate((n2_t, n2_t, dy_t)):

            def tile_body(tile, carry, kind=kind, source=source):
                cols = pl.ds(pl.multiple_of(tile * WIDE, WIDE), WIDE)
                w3[kind, at, cols] = dot_nn(source[at, :], h3[kind, :, cols]).astype(jnp.bfloat16)
                return carry

            lax.fori_loop(0, units // WIDE, tile_body, 0)
        for far in (1, 0):
            for kind in range(3):
                over_c(kind, step, far).start()

    def over_c(kind, step, far):
        x_at = 1 - me_x if far else me_x
        return remote(
            w3.at[kind, row_block(ahead(step), x_at, 1 - me_c)],
            c_in.at[kind, step, far],
            c_send.at[kind, step, far],
            c_recv.at[kind, step, far],
            to_c,
        )

    def over_x(kind):
        return remote(
            w3.at[kind, row_block(ahead(1), 1 - me_x, me_c)],
            x_in.at[kind],
            x_send.at[kind],
            x_recv.at[kind],
            to_x,
        )

    out_copies = []

    def keep(kind, step, far, block):
        copy = pltpu.make_async_copy(
            block, sums_hbm.at[kind, step, far], out_sem.at[kind, step, far]
        )
        copy.start()
        out_copies.append(copy)

    def core_sums(step):
        for far in (1, 0):
            for kind in range(3):
                over_c(kind, step, far).wait_recv()
                x_at = 1 - me_x if far else me_x
                block = w3.at[kind, row_block(ahead(step), x_at, me_c)]
                add_rows(block, [c_in.at[kind, step, far]], block, rows)
                if step != 1:
                    keep(kind, step, far, block)
                elif far:
                    over_x(kind).start()

    def first_sums():
        for kind in range(3):
            over_x(kind).wait_recv()
            block = w3.at[kind, row_block(ahead(1), me_x, me_c)]
            add_rows(block, [x_in.at[kind]], block, rows)
            keep(kind, 1, 0, block)

    own_load.wait()
    w_loads(lambda copy: copy.wait())

    @pl.when(outer)
    def _():
        w3[:, :, main:] = jnp.zeros((3, width, units - main), jnp.bfloat16)

    chunk(0)
    forward(1)
    forward(2)
    ag_y_in(1).wait_recv()
    chunk(1)
    ag_y_in(2).wait_recv()
    ag_last().start()
    chunk(2)
    rs_step(1)
    ag_z_in(3).wait_recv()
    ag_last().wait_recv()
    chunk(3)
    rs_y(0).start()
    rs_step(2)
    grads(1)
    grads(2)
    core_sums(1)
    rs_step(3)
    grads(3)
    core_sums(2)
    grads(0)
    core_sums(3)
    rs_step(0)
    core_sums(0)

    cot_load = pltpu.make_async_copy(
        dy_hbm.at[0, mine], dy.at[pl.ds(0, own)], load_sem.at[z_size + 3]
    )
    cot_load.start()
    cot_load.wait()
    mid_load.wait()

    def mid_rows(index, total):
        at = pl.ds(pl.multiple_of(index * 32, 32), 32)
        grad, gain_sum = norm_back(mid[at, :], gain_ref[1:2, :], gm_ref[at, :])
        grad = grad + dy[at, :].astype(jnp.float32)
        gm_ref[at, :] = grad
        dy[pl.ds(pl.multiple_of(own + index * 32, 32), 32), :] = grad.astype(jnp.bfloat16)
        return total + gain_sum

    gain_sum = lax.fori_loop(0, own // 32, mid_rows, jnp.zeros((1, width), jnp.float32))
    gm_save = pltpu.make_async_copy(dy.at[pl.ds(own, own)], gm_hbm, load_sem.at[z_size + 3])
    gm_save.start()
    for index in range(4):
        gain_part[index : index + 1, :] = jnp.zeros((1, span), jnp.float32)
        gain_part[4 + index : 5 + index, :] = gain_sum[:, index * span : (index + 1) * span]
    first_sums()
    gm_save.wait()

    for copy in mix_copies[3:] + out_copies:
        copy.wait()
    for index in range(z_size):
        if index in (1, 2):
            ag_y(index).wait_send()
        if index == 3:
            ag_last().wait_send()
        rs_y(index).wait_send()
        if index < z_size - 1:
            ag_z(index).wait_send()
        if index:
            rs_z(index).wait_send()
        for kind in range(3):
            over_c(kind, index, 0).wait_send()
            over_c(kind, index, 1).wait_send()
            if index == 1:
                over_x(kind).wait_send()


def ffn_call(gains, normed, grad_all, weights, mid, rows, main):
    z_size = lax.axis_size("z")
    pair, width = normed.shape
    units = weights.shape[2]
    own = pair // 2
    wide = lambda *lead: pltpu.VMEM((*lead, width), jnp.bfloat16)
    tall = lambda *lead: pltpu.VMEM((*lead, width, own), jnp.bfloat16)
    dma = lambda *lead: pltpu.SemaphoreType.DMA(lead)
    vmem = pl.BlockSpec(memory_space=pltpu.VMEM)
    hbm = pl.BlockSpec(memory_space=pl.ANY)
    return pl.pallas_call(
        functools.partial(ffn_kernel, z_size, main),
        out_shape=(
            jax.ShapeDtypeStruct((own, width), jnp.float32),
            jax.ShapeDtypeStruct((8, width // z_size), jnp.float32),
            jax.ShapeDtypeStruct((z_size, 2, width, own), jnp.bfloat16),
            jax.ShapeDtypeStruct((3, z_size, 2, rows, units), jnp.bfloat16),
            jax.ShapeDtypeStruct((own, width), jnp.bfloat16),
        ),
        in_specs=[vmem, hbm, hbm, hbm, hbm],
        out_specs=(vmem, vmem, hbm, hbm, hbm),
        scratch_shapes=[
            wide(z_size, pair),
            wide(pair),
            pltpu.VMEM(weights.shape, jnp.bfloat16),
            pltpu.VMEM((3, z_size * pair, units), jnp.bfloat16),
            pltpu.VMEM((width, z_size * pair), jnp.bfloat16),
            pltpu.VMEM((width, z_size * pair), jnp.bfloat16),
            tall(z_size, 2),
            tall(2),
            tall(z_size),
            tall(z_size - 1),
            tall(z_size - 1),
            pltpu.VMEM((3, z_size, 2, rows, units), jnp.bfloat16),
            pltpu.VMEM((3, rows, units), jnp.bfloat16),
            pltpu.VMEM((own, width), jnp.float32),
            dma(z_size + 5),
            dma(z_size),
            dma(z_size),
            dma(z_size),
            dma(z_size),
            dma(z_size),
            dma(z_size),
            dma(z_size),
            dma(z_size),
            dma(z_size),
            dma(3, z_size, 2),
            dma(3, z_size, 2),
            dma(3),
            dma(3),
            dma(3, z_size, 2),
        ],
        compiler_params=pltpu.CompilerParams(
            collective_id=0, has_side_effects=True, vmem_limit_bytes=VMEM_BYTES
        ),
        cost_estimate=pl.CostEstimate(
            flops=18 * z_size * pair * width * units,
            bytes_accessed=4 * weights.size + 12 * z_size * pair * width,
            transcendentals=z_size * pair * units,
        ),
    )(gains, normed, grad_all, weights, mid)


def spin(values, table):
    first = values[:, : values.shape[1] // 2]
    turned = first * table[0] + pltpu.roll(first, first.shape[1] // 2, 1) * table[1]
    return jnp.concatenate([turned, values[:, values.shape[1] // 2 :]], axis=1)


def spin_back(values, table):
    first = values[:, : values.shape[1] // 2]
    turned = first * table[0] - pltpu.roll(first, first.shape[1] // 2, 1) * table[1]
    return jnp.concatenate([turned, values[:, values.shape[1] // 2 :]], axis=1)


def head_probs(rotated, keys, allowed):
    scores = jnp.where(allowed > 0.5, matmul_nt(rotated, keys), masked_score)
    weights = jnp.exp(scores - jnp.max(scores, axis=-1, keepdims=True))
    return weights / jnp.sum(weights, axis=-1, keepdims=True)


def ragged_split(columns, parts):
    main = columns // parts // 128 * 128
    return main, main + 128


def pre_kernel(
    z_size,
    tok_ref,
    wkv_ref,
    gains_ref,
    table_ref,
    seg_ref,
    cot_hbm,
    wq_hbm,
    wo_hbm,
    wg_hbm,
    wu_hbm,
    wd_hbm,
    n1_ref,
    rot_ref,
    key_ref,
    val_ref,
    att_ref,
    mid_ref,
    n2_ref,
    gain_ref,
    allow_ref,
    kv_out,
    wq_out,
    wo_out,
    w3_out,
    dy_out,
    kv_w,
    q_w,
    o_w,
    tok,
    part,
    part_y,
    query,
    y_send,
    y_recv,
    ky_send,
    ky_recv,
    az_send,
    az_recv,
    ax_send,
    ax_recv,
    ac_send,
    ac_recv,
    fz_send,
    fz_recv,
    fx_send,
    fx_recv,
    fc_send,
    fc_recv,
    dz_send,
    dz_recv,
    dy_send,
    dy_recv,
    local_sem,
):
    me_z, me_x = lax.axis_index("z"), lax.axis_index("x")
    me_c, me_y = lax.axis_index("c"), lax.axis_index("mp")
    own, width = tok_ref.shape
    rows = wq_hbm.shape[0]
    half_rows = wkv_ref.shape[0]
    head = key_ref.shape[1]
    main, units = ragged_split(wg_hbm.shape[1], z_size)
    to_y, to_x, to_c = {"mp": 1 - me_y}, {"x": 1 - me_x}, {"c": 1 - me_c}

    def to_z(step):
        return {"z": lax.rem(me_z + step, z_size)}

    def from_z(step):
        return lax.rem(me_z - step + z_size, z_size)

    def row_block(step, x_at, c_at):
        start = ((from_z(step) * 2 + x_at) * 2 + c_at) * rows
        return pl.ds(pl.multiple_of(start, rows), rows)

    mine = pl.ds(pl.multiple_of(me_y * own, own), own)
    theirs = pl.ds(pl.multiple_of((1 - me_y) * own, own), own)
    bufs = (kv_w, q_w, o_w)
    inputs = (None, wq_hbm, wo_hbm)

    locals_ = []

    def local(src, dst):
        copy = pltpu.make_async_copy(src, dst, local_sem.at[len(locals_)])
        copy.start()
        locals_.append(copy)
        return copy

    here = row_block(0, me_x, me_c)
    own_q = local(wq_hbm, q_w.at[here])
    own_o = local(wo_hbm, o_w.at[here])
    ffn_in = (wg_hbm, wu_hbm, wd_hbm)

    def body_of(target):
        return pl.ds(pl.multiple_of(target * main, 128), main), pl.ds(0, main)

    def tail_of(target):
        start = z_size * main + lax.rem(target + 1, 2) * 128
        return pl.ds(pl.multiple_of(start, 128), 128), pl.ds(main, 128)

    def is_inner(at):
        return (at > 0) & (at < z_size - 1)

    own_f = []
    for kind in range(3):
        src, dst = body_of(me_z)
        own_f.append(local(ffn_in[kind].at[:, src], w3_out.at[kind, here, dst]))

    def own_tail(kind):
        src, dst = tail_of(me_z)
        return pltpu.make_async_copy(
            ffn_in[kind].at[:, src], w3_out.at[kind, here, dst], local_sem.at[12 + kind]
        )

    @pl.when(is_inner(me_z))
    def _():
        for kind in range(3):
            own_tail(kind).start()
    own_d = local(cot_hbm, dy_out.at[0, mine])

    kv_own = pl.ds(pl.multiple_of(here.start + me_y * half_rows, half_rows), half_rows)
    spread = jnp.concatenate([gains_ref[...], jnp.zeros((120, 128), jnp.float32)], axis=0).T
    kv_w[kv_own, : 2 * head] = wkv_ref[...]
    kv_w[kv_own, 2 * head :] = spread[:half_rows, :].astype(jnp.bfloat16)

    barrier = pltpu.get_barrier_semaphore()
    peers = [to_y, to_x, to_c] + [to_z(step) for step in range(1, z_size)]
    for where in peers:
        pl.semaphore_signal(barrier, inc=1, device_id=where, device_id_type=MESH_ID)
    pl.semaphore_wait(barrier, len(peers))

    tok_y = remote(tok_ref, tok.at[mine], y_send.at[1], y_recv.at[1], to_y)
    tok_y_in = remote(tok_ref, tok.at[theirs], y_send.at[1], y_recv.at[1], to_y)
    part_out = remote(part.at[theirs], part_y, y_send.at[2], y_recv.at[2], to_y)
    n2_y = remote(n2_ref.at[mine], n2_ref.at[mine], y_send.at[3], y_recv.at[3], to_y)
    n2_y_in = remote(n2_ref.at[theirs], n2_ref.at[theirs], y_send.at[3], y_recv.at[3], to_y)

    def block_of(kind, step, x_at):
        if kind:
            return row_block(step, x_at, me_c)
        return kv_rows(step, x_at, me_y)

    def kv_rows(step, x_at, y_at):
        start = row_block(step, x_at, me_c).start + y_at * half_rows
        return pl.ds(pl.multiple_of(start, half_rows), half_rows)

    def kv_y(step, far):
        x_at = 1 - me_x if far else me_x
        block = kv_w.at[kv_rows(step, x_at, me_y)]
        slot = step + z_size * far
        return remote(block, block, ky_send.at[slot], ky_recv.at[slot], to_y)

    def kv_y_in(step, far):
        x_at = 1 - me_x if far else me_x
        block = kv_w.at[kv_rows(step, x_at, 1 - me_y)]
        slot = step + z_size * far
        return remote(block, block, ky_send.at[slot], ky_recv.at[slot], to_y)

    def source(kind, step):
        if isinstance(step, int) and step == 0 and kind:
            return inputs[kind]
        return bufs[kind].at[block_of(kind, step, me_x)]

    first_z, last_z = (z_size - 1 - me_z) // (z_size - 1), me_z // (z_size - 1)
    inner = first_z + last_z == 0
    order = (0, 1 + 2 * first_z, 3 - first_z - last_z, 2 - first_z + last_z)
    hops = (
        None,
        (lax.rem(me_z + 1, z_size), 2),
        (lax.rem(me_z + z_size - 1, z_size), 2),
        (lax.rem(3 * (me_z + 3), z_size), lax.rem(2 * me_z + 3, z_size)),
    )

    def a_z_own(kind, right):
        return remote(
            source(kind, 0),
            bufs[kind].at[block_of(kind, 0, me_x)],
            az_send.at[kind, right],
            az_recv.at[kind, 1 if right else z_size - 1],
            to_z(1 if right else z_size - 1),
        )

    def a_z_start(kind):
        @pl.when(last_z == 0)
        def _():
            a_z_own(kind, 1).start()

        @pl.when(first_z == 0)
        def _():
            a_z_own(kind, 0).start()

    def a_z(kind, index):
        target, slot = hops[index]
        block = bufs[kind].at[block_of(kind, order[index], me_x)]
        return remote(
            block, block, az_send.at[kind, 1 + index], az_recv.at[kind, slot], {"z": target}
        )

    def a_z_next(kind, index):
        @pl.when(inner)
        def _():
            a_z(kind, index).start()

    def a_z_done(kind):
        @pl.when(last_z == 0)
        def _():
            a_z_own(kind, 1).wait_send()

        @pl.when(first_z == 0)
        def _():
            a_z_own(kind, 0).wait_send()

        @pl.when(inner)
        def _():
            for index in range(1, z_size):
                a_z(kind, index).wait_send()

    def a_z_in(kind, step):
        block = bufs[kind].at[block_of(kind, step, me_x)]
        return remote(block, block, az_send.at[kind, 0], az_recv.at[kind, step], to_z(1))

    def a_x(kind, step):
        return remote(
            source(kind, step),
            bufs[kind].at[block_of(kind, step, me_x)],
            ax_send.at[kind, step],
            ax_recv.at[kind, step],
            to_x,
        )

    def a_x_in(kind, step):
        block = bufs[kind].at[block_of(kind, step, 1 - me_x)]
        return remote(block, block, ax_send.at[kind, step], ax_recv.at[kind, step], to_x)

    def a_c(kind, step, far):
        x_at = 1 - me_x if far else me_x
        block = bufs[kind].at[row_block(step, x_at, me_c)]
        src = source(kind, step) if kind and not far else block
        slot = step + z_size * far
        return remote(src, block, ac_send.at[kind, slot], ac_recv.at[kind, slot], to_c)

    def a_c_in(kind, step, far):
        x_at = 1 - me_x if far else me_x
        block = bufs[kind].at[row_block(step, x_at, 1 - me_c)]
        slot = step + z_size * far
        return remote(block, block, ac_send.at[kind, slot], ac_recv.at[kind, slot], to_c)

    def f_z(kind, step, act):
        target = lax.rem(me_z + step, z_size)

        def piece(index, src, dst):
            return remote(
                ffn_in[kind].at[:, src],
                w3_out.at[kind, here, dst],
                fz_send.at[kind, step, index],
                fz_recv.at[kind, step, index],
                to_z(step),
            )

        act(piece(0, *body_of(target)))

        @pl.when(is_inner(target))
        def _():
            act(piece(1, *tail_of(target)))

    def f_z_wait(kind, step):
        block = row_block(step, me_x, me_c)

        def piece(index, dst):
            part = w3_out.at[kind, block, dst]
            return remote(
                part, part, fz_send.at[kind, step, index], fz_recv.at[kind, step, index], to_z(step)
            )

        piece(0, pl.ds(0, main)).wait_recv()

        @pl.when(inner)
        def _():
            piece(1, pl.ds(main, 128)).wait_recv()

    def f_x(kind, step, x_at, act):
        for case, columns in ((inner, units), (first_z + last_z > 0, main)):

            @pl.when(case)
            def _(columns=columns):
                block = w3_out.at[kind, row_block(step, x_at, me_c), pl.ds(0, columns)]
                act(remote(block, block, fx_send.at[kind, step], fx_recv.at[kind, step], to_x))

    def f_x_start(kind, step):
        f_x(kind, step, me_x, lambda copy: copy.start())

    def f_x_wait(kind, step):
        f_x(kind, step, 1 - me_x, lambda copy: copy.wait_recv())

    def f_x_done(kind, step):
        f_x(kind, step, me_x, lambda copy: copy.wait_send())

    def f_c(kind, step, far):
        block = w3_out.at[kind, row_block(step, 1 - me_x if far else me_x, me_c)]
        slot = step + z_size * far
        return remote(block, block, fc_send.at[kind, slot], fc_recv.at[kind, slot], to_c)

    def f_c_in(kind, step, far):
        block = w3_out.at[kind, row_block(step, 1 - me_x if far else me_x, 1 - me_c)]
        slot = step + z_size * far
        return remote(block, block, fc_send.at[kind, slot], fc_recv.at[kind, slot], to_c)

    def d_source(step):
        return cot_hbm if isinstance(step, int) else dy_out.at[step, mine]

    def d_z_own(right):
        slot = 1 if right else z_size - 1
        return remote(
            cot_hbm, dy_out.at[slot, mine], dz_send.at[right], dz_recv.at[slot], to_z(slot)
        )

    def d_z(index):
        target, slot = hops[index]
        return remote(
            dy_out.at[order[index], mine],
            dy_out.at[slot, mine],
            dz_send.at[1 + index],
            dz_recv.at[slot],
            {"z": target},
        )

    def d_z_done():
        @pl.when(last_z == 0)
        def _():
            d_z_own(1).wait_send()

        @pl.when(first_z == 0)
        def _():
            d_z_own(0).wait_send()

        @pl.when(inner)
        def _():
            for index in range(1, z_size):
                d_z(index).wait_send()

    def d_z_in(step):
        block = dy_out.at[step, mine]
        return remote(block, block, dz_send.at[0], dz_recv.at[step], to_z(1))

    def d_y(step):
        return remote(
            d_source(step), dy_out.at[step, mine], dy_send.at[step], dy_recv.at[step], to_y
        )

    def d_y_in(step):
        block = dy_out.at[step, theirs]
        return remote(block, block, dy_send.at[step], dy_recv.at[step], to_y)

    for kind in (1, 0, 2):
        a_z_start(kind)
        a_x(kind, 0).start()
    kv_y(0, 0).start()
    tok_y.start()
    for kind in (1, 2):
        a_c(kind, 0, 0).start()

    for at_end, away in ((first_z, 1), (last_z, z_size - 1)):

        @pl.when(at_end > 0)
        def _(away=away):
            d_z_own(1 if away == 1 else 0).start()
            for kind in range(3):
                f_z(kind, away, lambda copy: copy.start())

    tok[mine, :] = tok_ref[...]
    seq = 2 * own
    query_at = lax.broadcasted_iota(jnp.int32, (seq, seq), 0)
    key_at = lax.broadcasted_iota(jnp.int32, (seq, seq), 1)
    same = seg_ref[...].T[:, :1] == seg_ref[:1, :]
    allowed = same & (key_at <= query_at) & (query_at - key_at < WINDOW)
    allow_ref[...] = jnp.where(allowed, 1.0, 0.0)
    d_y(0).start()

    def from_x(index):
        step = order[index]
        for kind in (1, 0, 2):
            a_x_in(kind, step).wait_recv()
            if kind:
                a_c(kind, step, 1).start()
            else:
                kv_y(step, 1).start()

    def from_y(index):
        step = order[index]
        for far in range(2):
            kv_y_in(step, far).wait_recv()
            a_c(0, step, far).start()

    for index in range(1, z_size):
        step = order[index]
        for kind in (1, 0, 2):
            a_z_in(kind, step).wait_recv()
            a_z_next(kind, index)
            a_x(kind, step).start()
            if kind:
                a_c(kind, step, 0).start()
            else:
                kv_y(step, 0).start()
        if index == z_size - 1:

            @pl.when(inner)
            def _():
                d_z_own(1).start()
                d_z_own(0).start()

            for copy in own_f:
                copy.wait()

            @pl.when(inner)
            def _():
                for kind in range(3):
                    own_tail(kind).wait()

            for kind in range(3):
                for away, sent in ((1, first_z), (3, last_z), (2, 0)):

                    @pl.when(sent == 0 if away != 2 else me_z >= 0)
                    def _(kind=kind, away=away):
                        f_z(kind, away, lambda copy: copy.start())

            for kind in range(3):
                f_x_start(kind, 0)
                f_c(kind, 0, 0).start()
        if index >= 2:
            from_x(index - 2)
            from_y(index - 2)
    for index in (z_size - 2, z_size - 1):
        from_x(index)
        from_y(index)

    def hand_on(kind, step):
        f_z_wait(kind, step)
        f_x_start(kind, step)
        f_c(kind, step, 0).start()

    def cross(kind, step):
        f_x_wait(kind, step)
        f_c(kind, step, 1).start()

    def pass_cotangent(step):
        d_z_in(order[step]).wait_recv()

        @pl.when(inner)
        def _():
            d_z(step).start()

        d_y(order[step]).start()

    def pass_if(case, step):
        @pl.when(case)
        def _():
            pass_cotangent(step)

    outer = first_z + last_z > 0
    pass_cotangent(1)
    pass_if(inner, 2)
    tok_y_in.wait_recv()
    own_q.wait()
    own_o.wait()
    for kind in (0, 1):
        for step in range(z_size):
            for far in range(2):
                a_c_in(kind, step, far).wait_recv()

    gains = kv_w[:, 2 * head :].astype(jnp.float32).T[:8, :]
    gain_ref[...] = gains

    def norm_rows(index, carry):
        at = pl.ds(pl.multiple_of(index * 32, 32), 32)
        values = tok[at, :].astype(jnp.float32)
        scale = lax.rsqrt(jnp.mean(values * values, axis=-1, keepdims=True) + epsilon)
        n1_ref[at, :] = (values * scale * gain_ref[0:1, :]).astype(jnp.bfloat16)
        return carry

    lax.fori_loop(0, 2 * own // 32, norm_rows, 0)
    hand_on(0, order[1])
    table = (table_ref[0], table_ref[1])
    key_ref[...] = spin(dot_nn(n1_ref[...], kv_w[:, :head]), table).astype(jnp.bfloat16)
    val_ref[...] = dot_nn(n1_ref[...], kv_w[:, head : 2 * head]).astype(jnp.bfloat16)
    hand_on(0, order[2])
    head_scale = head ** (-0.5)
    heads = att_ref.shape[1] // head

    half_cols = att_ref.shape[1] // 2
    for index in range(2):
        cols = pl.ds(index * half_cols, half_cols)
        query[:, cols] = dot_nn(n1_ref[...], q_w[:, cols])

    def attend(index):
        cols = pl.ds(index * head, head)
        rotated = (spin(query[:, cols], table) * head_scale).astype(jnp.bfloat16)
        rot_ref[:, cols] = rotated
        probs = head_probs(rotated, key_ref[...], allow_ref[...]).astype(jnp.bfloat16)
        att_ref[:, cols] = dot_nn(probs, val_ref[...]).astype(jnp.bfloat16)

    tasks = [
        lambda: hand_on(0, order[3]),
        lambda: cross(0, 0),
        lambda: hand_on(1, order[1]),
        lambda: (cross(1, 0), pass_if(inner, 3)),
        lambda: (cross(2, 0), hand_on(1, order[2])),
    ]
    for index in range(heads):
        attend(index)
        if index < len(tasks):
            tasks[index]()
    for step in range(z_size):
        for far in range(2):
            a_c_in(2, step, far).wait_recv()
    saves = [
        local(kv_w, kv_out),
        local(q_w, wq_out),
        local(o_w, wo_out),
    ]
    span = width // 4

    def project(index, carry):
        cols = pl.ds(pl.multiple_of(index * span, span), span)
        part[:, cols] = matmul_nt(att_ref[...], o_w[cols, :]).astype(jnp.bfloat16)
        return carry

    lax.fori_loop(0, 4, project, 0)
    part_out.start()
    hand_on(1, order[3])
    pass_if(outer, 2)
    cross(0, order[1])
    hand_on(2, order[1])
    part_out.wait_recv()

    def middle(index, carry):
        at = pl.ds(pl.multiple_of(index * 32, 32), 32)
        there = pl.ds(pl.multiple_of(me_y * own + index * 32, 32), 32)
        values = (
            tok_ref[at, :].astype(jnp.float32)
            + part[there, :].astype(jnp.float32)
            + part_y[at, :].astype(jnp.float32)
        )
        mid_ref[at, :] = values
        scale = lax.rsqrt(jnp.mean(values * values, axis=-1, keepdims=True) + epsilon)
        n2_ref[there, :] = (values * scale * gain_ref[1:2, :]).astype(jnp.bfloat16)
        return carry

    lax.fori_loop(0, own // 32, middle, 0)
    n2_y.start()
    hand_on(2, order[2])
    cross(0, order[2])
    cross(0, order[3])
    hand_on(2, order[3])
    pass_if(outer, 3)
    for kind in (1, 2):
        for index in (1, 2, 3):
            cross(kind, order[index])
    for kind in range(3):
        for step in range(z_size):
            for far in range(2):
                f_c_in(kind, step, far).wait_recv()
    for step in range(z_size):
        d_y_in(step).wait_recv()
    n2_y_in.wait_recv()

    for kind in range(3):
        a_z_done(kind)
    d_z_done()
    tok_y.wait_send()
    part_out.wait_send()
    n2_y.wait_send()
    own_d.wait()
    for copy in saves:
        copy.wait()
    for step in range(z_size):
        d_y(step).wait_send()
        for far in range(2):
            kv_y(step, far).wait_send()
        for kind in range(3):
            if step:
                f_z(kind, step, lambda copy: copy.wait_send())
            a_x(kind, step).wait_send()
            f_x_done(kind, step)
            for far in range(2):
                a_c(kind, step, far).wait_send()
                f_c(kind, step, far).wait_send()


def pre_call(tokens, w_kv, gains, table, segments, cotangent, w_query, w_out, ffn):
    z_size = lax.axis_size("z")
    own, width = tokens.shape
    seq = 2 * own
    rows, cols = w_query.shape
    head = table.shape[2] * 2
    units = ragged_split(ffn[0].shape[1], z_size)[1]
    low = lambda *dims: jax.ShapeDtypeStruct(dims, jnp.bfloat16)
    full = lambda *dims: jax.ShapeDtypeStruct(dims, jnp.float32)
    dma = lambda *lead: pltpu.SemaphoreType.DMA(lead)
    vmem = pl.BlockSpec(memory_space=pltpu.VMEM)
    hbm = pl.BlockSpec(memory_space=pl.ANY)
    wide = lambda *lead: pltpu.VMEM((*lead, width), jnp.bfloat16)
    return pl.pallas_call(
        functools.partial(pre_kernel, z_size),
        out_shape=(
            low(seq, width),
            low(seq, cols),
            low(seq, head),
            low(seq, head),
            low(seq, cols),
            full(own, width),
            low(seq, width),
            full(8, width),
            full(seq, seq),
            low(width, 2 * head + 128),
            low(width, cols),
            low(width, cols),
            low(3, width, units),
            low(z_size, seq, width),
        ),
        in_specs=[vmem] * 5 + [hbm] * 6,
        out_specs=(vmem,) * 9 + (hbm,) * 5,
        scratch_shapes=[
            pltpu.VMEM((width, 2 * head + 128), jnp.bfloat16),
            pltpu.VMEM((width, cols), jnp.bfloat16),
            pltpu.VMEM((width, cols), jnp.bfloat16),
            wide(seq),
            wide(seq),
            wide(own),
            pltpu.VMEM((seq, cols), jnp.float32),
            dma(4),
            dma(4),
            dma(2 * z_size),
            dma(2 * z_size),
            dma(3, z_size + 1),
            dma(3, z_size),
            dma(3, z_size),
            dma(3, z_size),
            dma(3, 2 * z_size),
            dma(3, 2 * z_size),
            dma(3, z_size, 2),
            dma(3, z_size, 2),
            dma(3, z_size),
            dma(3, z_size),
            dma(3, 2 * z_size),
            dma(3, 2 * z_size),
            dma(z_size + 1),
            dma(z_size),
            dma(z_size),
            dma(z_size),
            dma(16),
        ],
        compiler_params=pltpu.CompilerParams(
            collective_id=1, has_side_effects=True, vmem_limit_bytes=VMEM_BYTES
        ),
        cost_estimate=pl.CostEstimate(
            flops=8 * seq * width * cols,
            bytes_accessed=8 * width * (cols + units),
            transcendentals=seq * seq * cols // head,
        ),
    )(tokens, w_kv, gains, table, segments, cotangent, w_query, w_out, *ffn)


def post_kernel(
    z_size,
    main,
    tok_ref,
    gain_ref,
    gain_part_ref,
    n1_ref,
    rot_ref,
    key_ref,
    val_ref,
    att_ref,
    table_ref,
    allow_ref,
    kv_hbm,
    wq_hbm,
    wo_hbm,
    mix_hbm,
    gmf_hbm,
    gmb_hbm,
    mid_hbm,
    sums_hbm,
    mixed_ref,
    tgrad_ref,
    gsum_ref,
    kvg_ref,
    qg_ref,
    og_ref,
    ffn_out,
    kv_w,
    q_w,
    o_w,
    o_part,
    gm,
    gm_f,
    gq,
    gkv,
    kv_sum,
    back_y,
    mix_y,
    mix_z,
    mix_s,
    o_c,
    o_x,
    o_z,
    q_c,
    q_x,
    q_z,
    kv_y,
    kv_c,
    kv_x,
    kv_z,
    gain_own,
    gain_in,
    ffn_in,
    ffn_own,
    load_sem,
    own_sem,
    fx_send,
    fx_recv,
    fz_send,
    fz_recv,
    y_send,
    y_recv,
    my_send,
    my_recv,
    mz_send,
    mz_recv,
    wc_send,
    wc_recv,
    wx_send,
    wx_recv,
    wz_send,
    wz_recv,
    kc_send,
    kc_recv,
    kz_send,
    kz_recv,
    g_send,
    g_recv,
):
    me_z, me_x = lax.axis_index("z"), lax.axis_index("x")
    me_c, me_y = lax.axis_index("c"), lax.axis_index("mp")
    own, width = tok_ref.shape
    seq = 2 * own
    head = key_ref.shape[1]
    cols_here = att_ref.shape[1]
    heads = cols_here // head
    rows = qg_ref.shape[0]
    span = width // z_size
    mine = pl.ds(pl.multiple_of(me_y * own, own), own)
    theirs = pl.ds(pl.multiple_of((1 - me_y) * own, own), own)
    to_y, to_x, to_c = {"mp": 1 - me_y}, {"x": 1 - me_x}, {"c": 1 - me_c}
    head_scale = head ** (-0.5)

    def behind(step):
        return lax.rem(me_z - step + z_size, z_size)

    def to_z(step):
        return {"z": lax.rem(me_z + step, z_size)}

    def row_block(step, x_at, c_at):
        start = ((behind(step) * 2 + x_at) * 2 + c_at) * rows
        return pl.ds(pl.multiple_of(start, rows), rows)

    loads = [
        pltpu.make_async_copy(wo_hbm, o_w, load_sem.at[0]),
        pltpu.make_async_copy(wq_hbm, q_w, load_sem.at[1]),
        pltpu.make_async_copy(
            kv_hbm.at[:, :, :, :, :, pl.ds(0, 2 * head)], kv_w, load_sem.at[2]
        ),
    ]
    for step in range(z_size):
        loads.append(
            pltpu.make_async_copy(mix_hbm.at[step, me_y], mix_s.at[step], load_sem.at[3 + step])
        )
    loads.append(pltpu.make_async_copy(gmf_hbm, gm_f, load_sem.at[3 + z_size]))
    loads.append(pltpu.make_async_copy(gmb_hbm, gm.at[mine], load_sem.at[4 + z_size]))
    mid_load = pltpu.make_async_copy(mid_hbm, gm_f, load_sem.at[5 + z_size])
    for load in loads:
        load.start()

    barrier = pltpu.get_barrier_semaphore()
    peers = [to_y, to_x, to_c] + [to_z(step) for step in range(1, z_size)]
    for where in peers:
        pl.semaphore_signal(barrier, inc=1, device_id=where, device_id_type=MESH_ID)
    pl.semaphore_wait(barrier, len(peers))

    tasks = [(step, kind) for step in (2, 3) for kind in range(3)]

    def f_x(index):
        step, kind = tasks[index]
        return remote(
            sums_hbm.at[kind, step, 1],
            ffn_in.at[index],
            fx_send.at[index],
            fx_recv.at[index],
            to_x,
        )

    def f_own(index):
        step, kind = tasks[index]
        return pltpu.make_async_copy(
            sums_hbm.at[kind, step, 0], ffn_own.at[index % 2], own_sem.at[index % 2]
        )

    def f_z(step, kind, source_z, act):
        for case, columns in (
            ((source_z > 0) & (source_z < z_size - 1), ffn_out.shape[3]),
            ((source_z == 0) | (source_z == z_size - 1), main),
        ):

            @pl.when(case)
            def _(columns=columns):
                cols = pl.ds(0, columns)
                if step == 1:
                    src = sums_hbm.at[kind, 1, 0, :, cols]
                else:
                    src = ffn_in.at[tasks.index((step, kind)), :, cols]
                act(
                    remote(
                        src,
                        ffn_out.at[kind, step, :, cols],
                        fz_send.at[kind, step],
                        fz_recv.at[kind, step],
                        to_z(step),
                    )
                )

    def tick(index):
        step, kind = tasks[index]
        f_x(index).wait_recv()
        f_own(index).wait()
        block = ffn_in.at[index]
        add_rows(block, [ffn_own.at[index % 2]], block, rows)
        if index + 2 < len(tasks):
            f_own(index + 2).start()
        f_z(step, kind, me_z, lambda copy: copy.start())

    def f_x_own(kind):
        return remote(
            sums_hbm.at[kind, 0, 1],
            ffn_out.at[kind, 0],
            fx_send.at[len(tasks) + kind],
            fx_recv.at[len(tasks) + kind],
            to_x,
        )

    f_own(0).start()
    f_own(1).start()
    for index in range(len(tasks)):
        f_x(index).start()
    for kind in range(3):
        f_z(1, kind, me_z, lambda copy: copy.start())

    gm_y = remote(gmb_hbm, gm.at[mine], y_send.at[0], y_recv.at[0], to_y)
    gm_y_in = remote(gm.at[theirs], gm.at[theirs], y_send.at[0], y_recv.at[0], to_y)
    gm_y.start()

    first_z, last_z = (z_size - 1 - me_z) // (z_size - 1), me_z // (z_size - 1)
    inner = first_z + last_z == 0
    order = (
        0,
        1 + (me_z + 1) // 2,
        2 + (2 * me_z - 3) * (1 - first_z - last_z),
        3 - 2 * (me_z // 2),
    )
    right = (None, 1 - me_z // 2, (3 - me_z) * (2 - me_z) // 6 + me_z // 2 * (1 - last_z), 1 - me_z // 2)

    def hop_slot(index):
        step, way = order[index], right[index]
        return way * lax.rem(step + 1, z_size) + (1 - way) * (step - 1 + 4 * ((3 - step) // 2))

    def hop_target(index):
        return {"z": me_z + 2 * right[index] - 1}

    def mix_over_y(step):
        return remote(
            mix_hbm.at[step, 1 - me_y], mix_y.at[step], my_send.at[step], my_recv.at[step], to_y
        )

    def mix_over_z(index):
        slot = hop_slot(index)
        return remote(
            mix_s.at[order[index]],
            mix_z.at[slot],
            mz_send.at[index],
            mz_recv.at[slot],
            hop_target(index),
        )

    def mix_z_in(slot):
        return remote(mix_z.at[slot], mix_z.at[slot], mz_send.at[1], mz_recv.at[slot], to_z(1))

    def mix_add(step, others, last):
        def add_tile(tile, carry):
            at = pl.ds(pl.multiple_of(tile * TILE, TILE), TILE)
            total = mix_s[step, at, :].astype(jnp.float32)
            for other in others:
                total = total + other[at, :].astype(jnp.float32)
            if last:
                mixed_ref[:, at] = (gm_f[:, at] + total.T).astype(jnp.bfloat16)
            else:
                mix_s[step, at, :] = total.astype(jnp.bfloat16)
            return carry

        lax.fori_loop(0, width // TILE, add_tile, 0)

    def mix_step(index):
        step = order[index]
        mix_over_y(step).wait_recv()
        from_y = mix_y.at[step]
        if index:

            @pl.when(inner)
            def _():
                mix_z_in(step).wait_recv()
                mix_add(step, [from_y, mix_z.at[step]], False)

            @pl.when(first_z + last_z > 0)
            def _():
                mix_add(step, [from_y], False)

            mix_over_z(index).start()
        else:
            mid_load.wait()

            @pl.when(first_z == 0)
            def _():
                mix_z_in(0).wait_recv()

            @pl.when(last_z == 0)
            def _():
                mix_z_in(z_size).wait_recv()

            @pl.when(inner)
            def _():
                mix_add(0, [from_y, mix_z.at[0], mix_z.at[z_size]], True)

            @pl.when(first_z > 0)
            def _():
                mix_add(0, [from_y, mix_z.at[z_size]], True)

            @pl.when(last_z > 0)
            def _():
                mix_add(0, [from_y, mix_z.at[0]], True)

    for index in (1, 2, 3, 0):
        mix_over_y(order[index]).start()

    kinds = ((o_part, o_c, o_x, o_z, og_ref), (o_w, q_c, q_x, q_z, qg_ref))

    def w_c(kind, step, far):
        x_at = 1 - me_x if far else me_x
        return remote(
            kinds[kind][0].at[row_block(step, x_at, 1 - me_c)],
            kinds[kind][1].at[step, far],
            wc_send.at[kind, step, far],
            wc_recv.at[kind, step, far],
            to_c,
        )

    def w_x(kind, step):
        return remote(
            kinds[kind][0].at[row_block(step, 1 - me_x, me_c)],
            kinds[kind][2].at[step],
            wx_send.at[kind, step],
            wx_recv.at[kind, step],
            to_x,
        )

    def w_z(kind, index):
        step, slot = order[index], hop_slot(index)
        return remote(
            kinds[kind][0].at[row_block(step, me_x, me_c)],
            kinds[kind][3].at[slot],
            wz_send.at[kind, index],
            wz_recv.at[kind, slot],
            hop_target(index),
        )

    def w_z_in(kind, slot):
        block = kinds[kind][3].at[slot]
        return remote(block, block, wz_send.at[kind, 1], wz_recv.at[kind, slot], to_z(1))

    def w_x_stage(kind, index):
        step = order[index]
        w_c(kind, step, 1).wait_recv()
        block = kinds[kind][0].at[row_block(step, 1 - me_x, me_c)]
        add_rows(block, [kinds[kind][1].at[step, 1]], block, rows)
        w_x(kind, step).start()

    def w_z_stage(kind, index):
        part, from_c, from_x, from_z, result = kinds[kind]
        step = order[index]
        w_c(kind, step, 0).wait_recv()
        w_x(kind, step).wait_recv()
        block = part.at[row_block(step, me_x, me_c)]
        others = [from_c.at[step, 0], from_x.at[step]]
        if index:

            @pl.when(inner)
            def _():
                w_z_in(kind, step).wait_recv()
                add_rows(block, [*others, from_z.at[step]], block, rows)

            @pl.when(first_z + last_z > 0)
            def _():
                add_rows(block, others, block, rows)

            w_z(kind, index).start()
        else:

            @pl.when(first_z == 0)
            def _():
                w_z_in(kind, 0).wait_recv()

            @pl.when(last_z == 0)
            def _():
                w_z_in(kind, z_size).wait_recv()

            @pl.when(inner)
            def _():
                add_rows(block, [*others, from_z.at[0], from_z.at[z_size]], result, rows)

            @pl.when(first_z > 0)
            def _():
                add_rows(block, [*others, from_z.at[z_size]], result, rows)

            @pl.when(last_z > 0)
            def _():
                add_rows(block, [*others, from_z.at[0]], result, rows)

    def w_product(kind, index, left, values):
        step = order[index]
        at = pl.ds(pl.multiple_of(behind(step) * span, 128), span)
        turned = left[:, at].T

        def tile_body(tile, carry):
            cols = pl.ds(pl.multiple_of(tile * TILE, TILE), TILE)
            kinds[kind][0][at, cols] = dot_nn(turned, values[:, cols]).astype(jnp.bfloat16)
            return carry

        lax.fori_loop(0, cols_here // TILE, tile_body, 0)
        for far in (1, 0):
            w_c(kind, step, far).start()

    outer = first_z + last_z > 0

    def if_outer(act, *args):
        @pl.when(outer)
        def _():
            act(*args)

    def if_inner(act, *args):
        @pl.when(inner)
        def _():
            act(*args)

    tick(0)
    tick(1)
    loads[-1].wait()
    gm_y_in.wait_recv()
    w_product(0, 1, gm, att_ref)
    w_product(0, 2, gm, att_ref)
    w_x_stage(0, 1)
    tick(2)
    w_product(0, 3, gm, att_ref)
    w_x_stage(0, 2)
    w_product(0, 0, gm, att_ref)
    w_x_stage(0, 3)
    tick(3)
    for load in loads[:-1]:
        load.wait()
    if_outer(mix_step, 1)

    kv_sum[...] = jnp.zeros(kv_sum.shape, jnp.float32)
    table = (table_ref[0], table_ref[1])

    for index in range(2):
        cols = pl.ds(index * (cols_here // 2), cols_here // 2)
        gq[:, cols] = dot_nn(gm[...], o_w[:, cols]).astype(jnp.bfloat16)

    def attend_back(index):
        cols = pl.ds(index * head, head)
        grad_vals = gq[:, cols]
        rotated = rot_ref[:, cols]
        probs = head_probs(rotated, key_ref[...], allow_ref[...])
        grad_probs = matmul_nt(grad_vals, val_ref[...])
        delta = jnp.sum(probs * grad_probs, axis=-1, keepdims=True)
        grad_scores = (probs * (grad_probs - delta)).astype(jnp.bfloat16)
        grad_rot = dot_nn(grad_scores, key_ref[...])
        gq[:, cols] = (spin_back(grad_rot, table) * head_scale).astype(jnp.bfloat16)
        kv_sum[0] += matmul_tn(grad_scores, rotated)
        kv_sum[1] += matmul_tn(probs.astype(jnp.bfloat16), grad_vals)

    between = {
        0: lambda: (w_x_stage(0, 0), tick(4)),
        1: lambda: (tick(5), if_outer(mix_step, 2)),
        2: lambda: if_inner(mix_step, 1),
        4: lambda: (if_outer(mix_step, 3), if_outer(w_z_stage, 0, 1)),
    }
    for index in range(heads):
        attend_back(index)
        if index in between:
            between[index]()
    gkv[:, :head] = spin_back(kv_sum[0], table).astype(jnp.bfloat16)
    gkv[:, head:] = kv_sum[1].astype(jnp.bfloat16)

    w_product(1, 1, n1_ref, gq)
    w_product(1, 2, n1_ref, gq)
    w_x_stage(1, 1)
    w_product(1, 3, n1_ref, gq)
    w_x_stage(1, 2)
    if_outer(w_z_stage, 0, 2)
    w_product(1, 0, n1_ref, gq)
    w_x_stage(1, 3)
    w_x_stage(1, 0)
    for kind in range(3):
        f_x_own(kind).start()

    gm_y.wait_send()
    back = gm
    def input_tile(index, carry):
        at = pl.ds(pl.multiple_of(index * span, 128), span)
        back[:, at] = (
            matmul_nt(gq[...], q_w[at, :]) + matmul_nt(gkv[...], kv_w[index].reshape(span, 2 * head))
        ).astype(jnp.bfloat16)
        return carry

    lax.fori_loop(0, z_size, input_tile, 0)
    back_out = remote(back.at[theirs], back_y, y_send.at[1], y_recv.at[1], to_y)
    back_out.start()

    kv_part = kv_w

    def kv_tile(index, carry):
        at = pl.ds(pl.multiple_of(index * span, 128), span)
        product = dot_nn(n1_ref[:, at].T, gkv[...]).astype(jnp.bfloat16)
        kv_part[index] = product.reshape(kv_part.shape[1:])
        return carry

    lax.fori_loop(0, z_size, kv_tile, 0)
    kv_over_y = remote(kv_part.at[:, :, :, 1 - me_y], kv_y, y_send.at[2], y_recv.at[2], to_y)
    kv_over_y.start()
    if_outer(w_z_stage, 0, 3)
    if_inner(mix_step, 2)

    back_out.wait_recv()

    def input_rows(index, total):
        at = pl.ds(pl.multiple_of(index * 32, 32), 32)
        there = pl.ds(pl.multiple_of(me_y * own + index * 32, 32), 32)
        upstream = back[there, :].astype(jnp.float32) + back_y[at, :].astype(jnp.float32)
        grad, gain_part = norm_back(
            tok_ref[at, :].astype(jnp.float32), gain_ref[0:1, :], upstream
        )
        tgrad_ref[at, :] = (gm_f[at, :] + grad).astype(jnp.bfloat16)
        return total + gain_part

    attn_gain_part = lax.fori_loop(
        0, own // 32, input_rows, jnp.zeros((1, width), jnp.float32)
    )
    for index in range(4):
        at = slice(index * span, (index + 1) * span)
        gain_own[0, index : index + 1, :] = attn_gain_part[:, at]
        gain_own[0, 4 + index : 5 + index, :] = gain_part_ref[4 + index : 5 + index, :]

    def gain_send(stage, where):
        return remote(
            gain_own.at[stage], gain_in.at[stage], g_send.at[stage], g_recv.at[stage], where
        )

    gain_hops = [gain_send(0, to_y), gain_send(1, to_c), gain_send(2, to_x)]
    gain_last = [
        remote(
            gain_own.at[3], gain_in.at[2 + step], g_send.at[2 + step], g_recv.at[2 + step], to_z(step)
        )
        for step in range(1, z_size)
    ]

    def gain_fold(stage):
        gain_hops[stage].wait_recv()
        gain_own[stage + 1] = gain_own[stage] + gain_in[stage]

    gain_hops[0].start()
    mid_load.start()
    if_outer(w_z_stage, 1, 1)
    if_inner(mix_step, 3)
    if_outer(w_z_stage, 1, 2)
    gain_fold(0)
    gain_hops[1].start()
    if_outer(w_z_stage, 1, 3)
    if_inner(w_z_stage, 0, 1)
    gain_fold(1)
    gain_hops[2].start()
    kv_over_y.wait_recv()

    def kv_add_y(index, carry):
        for x_at in range(2):
            for c_at in range(2):
                block = kv_part.at[index, x_at, c_at, me_y]
                block[...] = (
                    block[...].astype(jnp.float32) + kv_y[index, x_at, c_at].astype(jnp.float32)
                ).astype(jnp.bfloat16)
        return carry

    lax.fori_loop(0, z_size, kv_add_y, 0)
    kv_over_c = remote(
        kv_part.at[:, :, 1 - me_c, me_y], kv_c, kc_send.at[0], kc_recv.at[0], to_c
    )
    kv_over_c.start()
    if_inner(w_z_stage, 0, 2)
    gain_fold(2)
    for copy in gain_last:
        copy.start()
    kv_over_c.wait_recv()

    def kv_add_c(index, carry):
        for x_at in range(2):
            block = kv_part.at[index, x_at, me_c, me_y]
            block[...] = (
                block[...].astype(jnp.float32) + kv_c[index, x_at].astype(jnp.float32)
            ).astype(jnp.bfloat16)
        return carry

    lax.fori_loop(0, z_size, kv_add_c, 0)
    kv_over_x = remote(
        kv_part.at[:, 1 - me_x, me_c, me_y], kv_x, kc_send.at[1], kc_recv.at[1], to_x
    )
    kv_over_x.start()
    if_inner(w_z_stage, 0, 3)
    if_inner(w_z_stage, 1, 1)
    mix_step(0)
    kv_over_x.wait_recv()

    def kv_add_x(index, carry):
        block = kv_part.at[index, me_x, me_c, me_y]
        block[...] = (
            block[...].astype(jnp.float32) + kv_x[index].astype(jnp.float32)
        ).astype(jnp.bfloat16)
        return carry

    lax.fori_loop(0, z_size, kv_add_x, 0)
    kv_over_z = [
        remote(
            kv_part.at[lax.rem(me_z + step, z_size), me_x, me_c, me_y],
            kv_z.at[step - 1],
            kz_send.at[step],
            kz_recv.at[step],
            to_z(step),
        )
        for step in range(1, z_size)
    ]
    for copy in kv_over_z:
        copy.start()
    if_inner(w_z_stage, 1, 2)
    w_z_stage(0, 0)
    if_inner(w_z_stage, 1, 3)
    w_z_stage(1, 0)
    for copy in gain_last:
        copy.wait_recv()
    gsum_ref[...] = gain_own[3] + gain_in[3] + gain_in[4] + gain_in[5]
    for copy in kv_over_z:
        copy.wait_recv()
    kvg_ref[...] = (
        kv_part[me_z, me_x, me_c, me_y].astype(jnp.float32)
        + kv_z[0].astype(jnp.float32)
        + kv_z[1].astype(jnp.float32)
        + kv_z[2].astype(jnp.float32)
    )

    back_out.wait_send()
    kv_over_y.wait_send()
    kv_over_c.wait_send()
    kv_over_x.wait_send()
    for kind in range(3):
        f_x_own(kind).wait()
    for index in range(len(tasks)):
        f_x(index).wait_send()
    for step in range(1, z_size):
        for kind in range(3):
            f_z(step, kind, me_z, lambda copy: copy.wait_send())
            f_z(step, kind, behind(step), lambda copy: copy.wait_recv())
    for copy in gain_hops + gain_last + kv_over_z:
        copy.wait_send()
    for step in range(z_size):
        mix_over_y(step).wait_send()
        if step:
            mix_over_z(step).wait_send()
        for kind in range(2):
            w_c(kind, step, 0).wait_send()
            w_c(kind, step, 1).wait_send()
            w_x(kind, step).wait_send()
            if step:
                w_z(kind, step).wait_send()


def post_call(
    tokens,
    gains,
    gain_part,
    normed_one,
    rotated,
    keys,
    values,
    attn_vals,
    table,
    allowed,
    kv_weight,
    query_weight,
    out_weight,
    mix_parts,
    grad_mid,
    grad_mid_low,
    mid,
    ffn_sums,
    main,
):
    z_size = lax.axis_size("z")
    own, width = tokens.shape
    seq = 2 * own
    head = keys.shape[1]
    cols = attn_vals.shape[1]
    rows = width // (4 * z_size)
    units = ffn_sums.shape[4]
    low = lambda *dims: pltpu.VMEM(dims, jnp.bfloat16)
    full = lambda *dims: pltpu.VMEM(dims, jnp.float32)
    out_full = lambda *dims: jax.ShapeDtypeStruct(dims, jnp.float32)
    out_low = lambda *dims: jax.ShapeDtypeStruct(dims, jnp.bfloat16)
    dma = lambda *lead: pltpu.SemaphoreType.DMA(lead)
    vmem = pl.BlockSpec(memory_space=pltpu.VMEM)
    hbm = pl.BlockSpec(memory_space=pl.ANY)
    z = z_size
    return pl.pallas_call(
        functools.partial(post_kernel, z_size, main),
        out_shape=(
            out_low(own, width),
            out_low(own, width),
            out_full(8, width // z),
            out_full(rows // 2, 2 * head),
            out_full(rows, cols),
            out_full(rows, cols),
            out_low(3, z, rows, units),
        ),
        in_specs=[vmem] * 10 + [hbm] * 8,
        out_specs=(vmem,) * 6 + (hbm,),
        scratch_shapes=[
            low(z, 2, 2, 2, rows // 2, 2 * head),
            low(width, cols),
            low(width, cols),
            low(width, cols),
            low(seq, width),
            full(own, width),
            low(seq, cols),
            low(seq, 2 * head),
            full(2, seq, head),
            low(own, width),
            low(z, width, own),
            low(z + 1, width, own),
            low(z, width, own),
            low(z, 2, rows, cols),
            low(z, rows, cols),
            low(z + 1, rows, cols),
            low(z, 2, rows, cols),
            low(z, rows, cols),
            low(z + 1, rows, cols),
            low(z, 2, 2, rows // 2, 2 * head),
            low(z, 2, rows // 2, 2 * head),
            low(z, rows // 2, 2 * head),
            low(z - 1, rows // 2, 2 * head),
            full(4, 8, width // z),
            full(6, 8, width // z),
            low(6, rows, units),
            low(2, rows, units),
            dma(6 + z),
            dma(2),
            dma(9),
            dma(9),
            dma(3, z),
            dma(3, z),
            dma(3),
            dma(3),
            dma(z),
            dma(z),
            dma(z),
            dma(z + 1),
            dma(2, z, 2),
            dma(2, z, 2),
            dma(2, z),
            dma(2, z),
            dma(2, z),
            dma(2, z + 1),
            dma(2),
            dma(2),
            dma(z),
            dma(z),
            dma(6),
            dma(6),
        ],
        compiler_params=pltpu.CompilerParams(
            collective_id=2, has_side_effects=True, vmem_limit_bytes=VMEM_BYTES
        ),
        cost_estimate=pl.CostEstimate(
            flops=14 * seq * width * cols,
            bytes_accessed=10 * width * cols,
            transcendentals=seq * seq * cols // head,
        ),
    )(
        tokens,
        gains,
        gain_part,
        normed_one,
        rotated,
        keys,
        values,
        attn_vals,
        table,
        allowed,
        kv_weight.reshape(z, 2, 2, 2, rows // 2, kv_weight.shape[1]),
        query_weight,
        out_weight,
        mix_parts,
        grad_mid,
        grad_mid_low,
        mid,
        ffn_sums,
    )


def layout_kernel(
    z_size,
    main,
    sum_ref,
    ffn_ref,
    q_ref,
    o_ref,
    kv_ref,
    mixed_in,
    tgrad_in,
    wg_ref,
    wu_ref,
    wd_ref,
    qg_ref,
    og_ref,
    kvg_ref,
    mixed_ref,
    tgrad_ref,
):
    me_z = lax.axis_index("z")
    for kind, out in enumerate((wg_ref, wu_ref, wd_ref)):
        for step in range(z_size):
            at = lax.rem(me_z - step + z_size, z_size)
            values = ffn_ref[kind, step].astype(jnp.float32)
            if step == 0:
                values = values + sum_ref[kind, 0, 0].astype(jnp.float32)
            body = pl.ds(pl.multiple_of(at * main, 128), main)
            out[:, body] = values[:, :main]

            @pl.when((at > 0) & (at < z_size - 1))
            def _(out=out, at=at, values=values):
                tail = z_size * main + lax.rem(at + 1, 2) * 128
                out[:, pl.ds(pl.multiple_of(tail, 128), 128)] = values[:, main:]
    qg_ref[...] = q_ref[...]
    og_ref[...] = o_ref[...]
    kvg_ref[...] = kv_ref[...]
    mixed_ref[...] = mixed_in[...]
    tgrad_ref[...] = tgrad_in[...]


def layout_call(ffn_sums, ffn_grads, query_grad, out_grad, kv_grad, mixed, tokens_grad, ffn_cols):
    z_size = lax.axis_size("z")
    main, units = ragged_split(ffn_cols, z_size)
    rows, cols = query_grad.shape
    parts = rows // 32
    kv_rows = kv_grad.shape[0] // parts
    full = lambda *dims: jax.ShapeDtypeStruct(dims, jnp.float32)
    row = lambda height, width: pl.BlockSpec((height, width), lambda index: (index, 0))
    own, width = mixed.shape
    share = pl.BlockSpec((own, width // parts), lambda index: (0, index))
    specs = [row(32, cols), row(32, cols), row(kv_rows, kv_grad.shape[1]), share, share]
    return pl.pallas_call(
        functools.partial(layout_kernel, z_size, main),
        grid=(parts,),
        out_shape=(
            *[full(rows, ffn_cols)] * 3,
            full(rows, cols),
            full(rows, cols),
            full(*kv_grad.shape),
            jax.ShapeDtypeStruct(mixed.shape, jnp.bfloat16),
            jax.ShapeDtypeStruct(mixed.shape, jnp.bfloat16),
        ),
        in_specs=[
            pl.BlockSpec((3, 1, 1, 32, units), lambda index: (0, 0, 0, index, 0)),
            pl.BlockSpec((3, z_size, 32, units), lambda index: (0, 0, index, 0)),
            *specs,
        ],
        out_specs=(*[row(32, ffn_cols)] * 3, *specs),
        compiler_params=pltpu.CompilerParams(vmem_limit_bytes=VMEM_BYTES),
    )(ffn_sums, ffn_grads, query_grad, out_grad, kv_grad, mixed, tokens_grad)


FF_SPLIT = 4


def ffn_pass(normed, grad_out, gate_weight, up_weight, down_weight):
    gate = jnp.dot(normed, gate_weight, preferred_element_type=jnp.float32)
    up_proj = jnp.dot(normed, up_weight, preferred_element_type=jnp.float32)
    grad_hidden = jnp.dot(grad_out, down_weight, preferred_element_type=jnp.float32)
    product, pull = jax.vjp(gelu_product, gate, up_proj)
    hidden = product.astype(jnp.bfloat16)
    grad_gate_f, grad_up_f = pull(grad_hidden)
    grad_gate = grad_gate_f.astype(jnp.bfloat16)
    grad_up = grad_up_f.astype(jnp.bfloat16)
    mixed_part = matmul_nt(hidden, down_weight).astype(jnp.bfloat16)
    normed_part = (matmul_nt(grad_gate, gate_weight) + matmul_nt(grad_up, up_weight)).astype(
        jnp.bfloat16
    )
    weight_parts = [
        matmul_tn(normed, grad_gate).astype(jnp.bfloat16),
        matmul_tn(normed, grad_up).astype(jnp.bfloat16),
        matmul_tn(grad_out, hidden).astype(jnp.bfloat16),
    ]
    return mixed_part, normed_part, weight_parts


def shards_general(
    tokens,
    segments,
    positions,
    cotangent,
    attn_gain,
    ffn_gain,
    w_kv,
    w_query,
    w_out,
    w_gate,
    w_up,
    w_down,
):
    everywhere = ("z", "xc", "mp")
    dp = ("z", "xc")
    z_size = lax.axis_size("z")
    xc_size = lax.axis_size("xc")
    gains = lax.all_gather(
        jnp.stack([attn_gain, ffn_gain], axis=1), everywhere, axis=0, tiled=True
    ).astype(jnp.float32)
    gain_one, gain_two = gains[:, 0], gains[:, 1]
    kv_weight = lax.all_gather(w_kv, everywhere, axis=0, tiled=True)
    head_dim = kv_weight.shape[1] // 2
    width = tokens.shape[1]
    seq_len = segments.shape[0]
    heads_here = w_query.shape[1] // head_dim
    scale = head_dim ** (-0.5)
    cosine, sine = rotary_angles(positions, head_dim)
    inputs_f = tokens.astype(jnp.float32)
    tokens_all = lax.all_gather(tokens, "mp", axis=0, tiled=True)
    normed_one = norm_gain(tokens_all.astype(jnp.float32), gain_one).astype(jnp.bfloat16)
    query_weight = lax.all_gather(w_query, dp, axis=0, tiled=True)
    out_weight = lax.all_gather(w_out, dp, axis=0, tiled=True)

    rows = w_gate.shape[0]
    unit = w_gate.shape[1] // z_size

    def spread(weight):
        pieces = weight.reshape(rows, z_size, unit).transpose(1, 0, 2)
        pieces = lax.all_to_all(pieces, "z", split_axis=0, concat_axis=0, tiled=True)
        return lax.all_gather(pieces, "xc", axis=1, tiled=False).reshape(width, unit)

    gate_weight, up_weight, down_weight = spread(w_gate), spread(w_up), spread(w_down)
    grad_all = lax.all_gather(cotangent, ("z", "mp"), axis=0, tiled=True)

    query = jnp.dot(normed_one, query_weight, preferred_element_type=jnp.float32).reshape(
        seq_len, heads_here, head_dim
    )
    rotated = (rotate(query, cosine[:, None], sine[:, None]) * scale).astype(jnp.bfloat16)
    keyval = jnp.dot(normed_one, kv_weight, preferred_element_type=jnp.float32)
    keys = rotate(keyval[:, :head_dim], cosine, sine).astype(jnp.bfloat16)
    values = keyval[:, head_dim:].astype(jnp.bfloat16)
    allowed = block_allowed(segments, 0, seq_len)
    scores = jnp.einsum("thd,sd->hts", rotated, keys, preferred_element_type=jnp.float32)
    scores = jnp.where(allowed[None], scores, masked_score)
    row_max = jnp.max(scores, axis=-1, keepdims=True)
    weights = jnp.exp(scores - row_max)
    probs = weights / jnp.sum(weights, axis=-1, keepdims=True)
    probs_low = probs.astype(jnp.bfloat16)
    attn_vals = (
        jnp.einsum("hts,sd->thd", probs_low, values, preferred_element_type=jnp.float32)
        .reshape(seq_len, heads_here * head_dim)
        .astype(jnp.bfloat16)
    )
    mid = inputs_f + lax.psum_scatter(
        matmul_nt(attn_vals, out_weight).astype(jnp.bfloat16),
        "mp",
        scatter_dimension=0,
        tiled=True,
    ).astype(jnp.float32)
    normed_two = norm_gain(mid, gain_two).astype(jnp.bfloat16)
    normed_all = lax.all_gather(normed_two, ("z", "mp"), axis=0, tiled=True)

    mixed_part, normed_part, weight_parts = ffn_pass(
        normed_all, grad_all, gate_weight, up_weight, down_weight
    )
    grad_normed_two = lax.psum_scatter(
        normed_part, ("z", "mp"), scatter_dimension=0, tiled=True
    ).astype(jnp.float32)
    mixed = (
        mid
        + lax.psum_scatter(mixed_part, ("z", "mp"), scatter_dimension=0, tiled=True).astype(
            jnp.float32
        )
    ).astype(jnp.bfloat16)

    def collect(part):
        pieces = part.reshape(z_size, xc_size, rows, unit).transpose(1, 0, 2, 3)
        pieces = pieces.reshape(xc_size * z_size * rows, unit)
        pieces = lax.psum_scatter(pieces, "xc", scatter_dimension=0, tiled=True)
        pieces = pieces.reshape(z_size, rows, unit)
        pieces = lax.all_to_all(pieces, "z", split_axis=0, concat_axis=0, tiled=True)
        return pieces.transpose(1, 0, 2).reshape(rows, z_size * unit).astype(jnp.float32)

    w_gate_grad, w_up_grad, w_down_grad = [collect(part) for part in weight_parts]

    norm_pull_two = jax.vjp(norm_gain, mid, gain_two)[1]
    grad_mid_norm, grad_gain_two = norm_pull_two(grad_normed_two)
    grad_mid = cotangent.astype(jnp.float32) + grad_mid_norm
    grad_mid_all = lax.all_gather(grad_mid.astype(jnp.bfloat16), "mp", axis=0, tiled=True)
    grad_vals = (
        jnp.dot(grad_mid_all, out_weight, preferred_element_type=jnp.float32)
        .astype(jnp.bfloat16)
        .reshape(seq_len, heads_here, head_dim)
    )
    grad_probs = jnp.einsum("thd,sd->hts", grad_vals, values, preferred_element_type=jnp.float32)
    delta = jnp.sum(probs * grad_probs, axis=-1, keepdims=True)
    grad_scores = (probs * (grad_probs - delta)).astype(jnp.bfloat16)
    grad_rot = jnp.einsum("hts,sd->thd", grad_scores, keys, preferred_element_type=jnp.float32)
    key_sum = jnp.einsum("hts,thd->sd", grad_scores, rotated, preferred_element_type=jnp.float32)
    value_sum = jnp.einsum("hts,thd->sd", probs_low, grad_vals, preferred_element_type=jnp.float32)
    grad_query = (
        (unrotate(grad_rot, cosine[:, None], sine[:, None]) * scale)
        .reshape(seq_len, heads_here * head_dim)
        .astype(jnp.bfloat16)
    )
    grad_kv = jnp.concatenate([unrotate(key_sum, cosine, sine), value_sum], axis=1).astype(
        jnp.bfloat16
    )
    grad_normed_one = lax.psum_scatter(
        (matmul_nt(grad_query, query_weight) + matmul_nt(grad_kv, kv_weight)).astype(jnp.bfloat16),
        "mp",
        scatter_dimension=0,
        tiled=True,
    ).astype(jnp.float32)
    norm_pull_one = jax.vjp(norm_gain, inputs_f, gain_one)[1]
    grad_input_norm, grad_gain_one = norm_pull_one(grad_normed_one)
    tokens_grad = (grad_mid + grad_input_norm).astype(jnp.bfloat16)

    w_query_grad = lax.psum_scatter(
        matmul_tn(normed_one, grad_query).astype(jnp.bfloat16), dp, scatter_dimension=0, tiled=True
    ).astype(jnp.float32)
    w_out_grad = lax.psum_scatter(
        matmul_tn(grad_mid_all, attn_vals).astype(jnp.bfloat16), dp, scatter_dimension=0, tiled=True
    ).astype(jnp.float32)
    small = jnp.concatenate(
        [matmul_tn(normed_one, grad_kv), grad_gain_one[:, None], grad_gain_two[:, None]], axis=1
    )
    small = lax.psum_scatter(small, everywhere, scatter_dimension=0, tiled=True)
    kv_grad = small[:, : 2 * head_dim]
    return (
        mixed,
        tokens_grad,
        small[:, 2 * head_dim],
        small[:, 2 * head_dim + 1],
        kv_grad,
        w_query_grad,
        w_out_grad,
        w_gate_grad,
        w_up_grad,
        w_down_grad,
    )


def shards_fast(
    tokens,
    segments,
    positions,
    cotangent,
    attn_gain,
    ffn_gain,
    w_kv,
    w_query,
    w_out,
    w_gate,
    w_up,
    w_down,
):
    seq_len = segments.shape[0]
    cosine, sine = rotary_angles(positions, w_kv.shape[1] // 2)
    table = jnp.stack(
        [
            jnp.concatenate([cosine, cosine], axis=1),
            jnp.concatenate([-sine, sine], axis=1),
        ]
    )
    gain_rows = jnp.pad(
        jnp.stack([attn_gain, ffn_gain]).astype(jnp.float32),
        ((0, 6), (0, 128 - attn_gain.shape[0])),
    )
    segment_rows = jnp.broadcast_to(segments.astype(jnp.float32)[None, :], (8, seq_len))
    (
        normed_one,
        rotated,
        keys,
        values,
        attn_vals,
        mid,
        normed_two,
        gains,
        allowed,
        kv_weight,
        query_weight,
        out_weight,
        ffn_weights,
        grad_all,
    ) = pre_call(
        tokens,
        w_kv,
        gain_rows,
        table,
        segment_rows,
        cotangent,
        w_query,
        w_out,
        (w_gate, w_up, w_down),
    )
    main = ragged_split(w_gate.shape[1], lax.axis_size("z"))[0]
    grad_mid, gain_part, mix_parts, ffn_sums, grad_mid_low = ffn_call(
        gains, normed_two, grad_all, ffn_weights, mid, w_gate.shape[0], main
    )
    mixed, tokens_grad, gain_grads, kv_grad, query_grad, out_grad, ffn_grads = post_call(
        tokens,
        gains,
        gain_part,
        normed_one,
        rotated,
        keys,
        values,
        attn_vals,
        table,
        allowed,
        kv_weight,
        query_weight,
        out_weight,
        mix_parts,
        grad_mid,
        grad_mid_low,
        mid,
        ffn_sums,
        main,
    )
    *ffn_out, query_grad, out_grad, kv_grad, mixed, tokens_grad = layout_call(
        ffn_sums,
        ffn_grads,
        query_grad,
        out_grad,
        kv_grad,
        mixed,
        tokens_grad,
        w_gate.shape[1],
    )
    share = attn_gain.shape[0]
    place = lax.axis_index(("z", "x", "c", "mp")) * share
    gain_grads = gain_grads.reshape(2, gain_grads.size // 2)
    gain_grads = lax.dynamic_slice(gain_grads, (0, place), (2, share))
    return (
        mixed,
        tokens_grad,
        gain_grads[0],
        gain_grads[1],
        kv_grad,
        query_grad,
        out_grad,
        *ffn_out,
    )


def solution(mesh):
    dp_size, mp_size = mesh.shape["dp"], mesh.shape["mp"]
    if dp_size == 4 * FF_SPLIT and mp_size == 2:
        body, dp = shards_fast, ("z", "x", "c")
        sizes = (FF_SPLIT, 2, 2, mp_size)
    else:
        body, dp = shards_general, ("z", "xc")
        sizes = (FF_SPLIT, dp_size // FF_SPLIT, mp_size)
    all_axes = (*dp, "mp")
    fine = jax.sharding.Mesh(mesh.devices.reshape(sizes), all_axes)
    in_specs = (
        P(all_axes, None),
        P(dp),
        P(dp),
        P(all_axes, None),
        P(all_axes),
        P(all_axes),
        P(all_axes, None),
        P(dp, "mp"),
        P(dp, "mp"),
        P(dp, "mp"),
        P(dp, "mp"),
        P(dp, "mp"),
    )
    out_specs = (
        P(all_axes, None),
        P(all_axes, None),
        P(all_axes),
        P(all_axes),
        P(all_axes, None),
        P(dp, "mp"),
        P(dp, "mp"),
        P(dp, "mp"),
        P(dp, "mp"),
        P(dp, "mp"),
    )
    return jax.shard_map(body, mesh=fine, in_specs=in_specs, out_specs=out_specs, check_vma=False)
```

```python
import functools

import jax
import jax.numpy as jnp
from jax import lax
from jax.experimental import pallas as pl
from jax.experimental.pallas import tpu as pltpu
from jax.sharding import PartitionSpec as P

WINDOW = 2048


epsilon = 1e-06
rope_base = 10000.0
masked_score = -1e30
VMEM_BYTES = 66_000_000


def norm_gain(values, gain):
    return values * lax.rsqrt(jnp.mean(values * values, axis=-1, keepdims=True) + epsilon) * gain


def rotary_angles(positions, head_width):
    quarter = head_width // 4
    freqs = rope_base ** (-jnp.arange(quarter).astype(jnp.float32) / quarter)
    phase = positions.astype(jnp.float32)[:, None] * freqs[None, :]
    return (jnp.cos(phase), jnp.sin(phase))


def rotate(values, cosine, sine):
    quarter = cosine.shape[-1]
    first_half = values[..., :quarter]
    second_half = values[..., quarter : 2 * quarter]
    return jnp.concatenate(
        [
            first_half * cosine - second_half * sine,
            second_half * cosine + first_half * sine,
            values[..., 2 * quarter :],
        ],
        axis=-1,
    )


def unrotate(values, cosine, sine):
    quarter = cosine.shape[-1]
    first_half = values[..., :quarter]
    second_half = values[..., quarter : 2 * quarter]
    return jnp.concatenate(
        [
            first_half * cosine + second_half * sine,
            second_half * cosine - first_half * sine,
            values[..., 2 * quarter :],
        ],
        axis=-1,
    )


def gelu_product(gate, up_proj):
    return jax.nn.gelu(gate, approximate=True) * up_proj


def matmul_nt(left, right):
    return lax.dot_general(
        left, right, (((1,), (1,)), ((), ())), preferred_element_type=jnp.float32
    )


def matmul_tn(left, right):
    return lax.dot_general(
        left, right, (((0,), (0,)), ((), ())), preferred_element_type=jnp.float32
    )


def block_allowed(segments, first_row, rows):
    seq_len = segments.shape[0]
    query_rows = first_row + jnp.arange(rows)
    key_rows = jnp.arange(seq_len)
    return (
        (segments[:, None] == segments[None, :])
        & (key_rows[None, :] <= query_rows[:, None])
        & (query_rows[:, None] - key_rows[None, :] < WINDOW)
    )


MESH_ID = pl.DeviceIdType.MESH
GELU_A = 0.7978845608028654
GELU_B = 0.044715
TILE = 256
WIDE = 512


def remote(src, dst, send_sem, recv_sem, where):
    return pltpu.make_async_remote_copy(
        src_ref=src,
        dst_ref=dst,
        send_sem=send_sem,
        recv_sem=recv_sem,
        device_id=where,
        device_id_type=MESH_ID,
    )


def dot_nn(left, right):
    return lax.dot_general(
        left, right, (((1,), (0,)), ((), ())), preferred_element_type=jnp.float32
    )


def gelu_parts(gate):
    square = gate * gate
    bend = jnp.tanh(GELU_A * gate * (1.0 + GELU_B * square))
    half = 0.5 * (1.0 + bend)
    slope = half + 0.5 * gate * (1.0 - bend * bend) * GELU_A * (1.0 + 3.0 * GELU_B * square)
    return gate * half, slope


def add_rows(first, rest, out, count):
    def body(index, carry):
        step = pl.ds(pl.multiple_of(index * 32, 32), 32)
        total = first[step, :].astype(jnp.float32)
        for other in rest:
            total = total + other[step, :].astype(jnp.float32)
        out[step, :] = total.astype(out.dtype)
        return carry

    lax.fori_loop(0, count // 32, body, 0)


def norm_back(values, gain, upstream):
    scale = lax.rsqrt(jnp.mean(values * values, axis=-1, keepdims=True) + epsilon)
    normed = values * scale
    pulled = gain * upstream
    back = scale * (pulled - normed * jnp.mean(normed * pulled, axis=-1, keepdims=True))
    return back, jnp.sum(upstream * normed, axis=0, keepdims=True)


def ffn_kernel(
    z_size,
    main,
    gain_ref,
    own_hbm,
    dy_hbm,
    w_hbm,
    mid_hbm,
    gm_ref,
    gain_part,
    mix_hbm,
    sums_hbm,
    gm_hbm,
    n2,
    dy,
    w3,
    h3,
    n2_t,
    dy_t,
    gn_part,
    mix_buf,
    gn_y,
    gn_z,
    gn_s,
    c_in,
    x_in,
    mid,
    load_sem,
    mix_sem,
    ag_y_send,
    ag_y_recv,
    ag_z_send,
    ag_z_recv,
    rs_y_send,
    rs_y_recv,
    rs_z_send,
    rs_z_recv,
    c_send,
    c_recv,
    x_send,
    x_recv,
    out_sem,
):
    own = own_hbm.shape[0] // 2
    width = own_hbm.shape[1]
    units = w3.shape[2]
    rows = c_in.shape[3]
    span = width // z_size
    me_y, me_z = lax.axis_index("mp"), lax.axis_index("z")
    me_x, me_c = lax.axis_index("x"), lax.axis_index("c")
    mine = pl.ds(pl.multiple_of(me_y * own, own), own)
    theirs = pl.ds(pl.multiple_of((1 - me_y) * own, own), own)
    to_y, to_x, to_c = {"mp": 1 - me_y}, {"x": 1 - me_x}, {"c": 1 - me_c}

    def ahead(step):
        return lax.rem(me_z + step, z_size)

    def to_z(step):
        return {"z": ahead(step)}

    def row_block(z_at, x_at, c_at):
        return pl.ds(pl.multiple_of(((z_at * 2 + x_at) * 2 + c_at) * rows, rows), rows)

    inner = (me_z > 0) & (me_z < z_size - 1)
    outer = (me_z == 0) | (me_z == z_size - 1)

    def w_load(index, columns):
        cols = pl.ds(0, columns)
        return pltpu.make_async_copy(
            w_hbm.at[index, :, cols], w3.at[index, :, cols], load_sem.at[z_size + index]
        )

    def w_loads(act):
        for case, columns in ((inner, units), (outer, main)):

            @pl.when(case)
            def _(columns=columns):
                for index in range(3):
                    act(w_load(index, columns))

    w_loads(lambda copy: copy.start())
    dy_loads = [
        pltpu.make_async_copy(dy_hbm.at[index], dy, load_sem.at[index])
        for index in range(z_size)
    ]
    own_load = pltpu.make_async_copy(own_hbm, n2.at[0], load_sem.at[z_size + 3])
    mid_load = pltpu.make_async_copy(mid_hbm, mid, load_sem.at[z_size + 4])
    for load in (own_load, dy_loads[0], mid_load):
        load.start()

    barrier = pltpu.get_barrier_semaphore()
    peers = [to_y, to_x, to_c] + [to_z(step) for step in range(1, z_size)]
    for where in peers:
        pl.semaphore_signal(barrier, inc=1, device_id=where, device_id_type=MESH_ID)
    pl.semaphore_wait(barrier, len(peers))

    def ag_y(index):
        block = n2.at[index, mine]
        return remote(block, block, ag_y_send.at[index], ag_y_recv.at[index], to_y)

    def ag_y_in(index):
        block = n2.at[index, theirs]
        return remote(block, block, ag_y_send.at[index], ag_y_recv.at[index], to_y)

    def ag_z(index):
        src = own_hbm.at[mine] if index == 0 else n2.at[index, mine]
        return remote(
            src, n2.at[index + 1, mine], ag_z_send.at[index], ag_z_recv.at[index + 1], to_z(1)
        )

    def ag_z_in(index):
        block = n2.at[index, mine]
        return remote(block, block, ag_z_send.at[0], ag_z_recv.at[index], to_z(1))

    def ag_last():
        return remote(
            n2.at[2, theirs], n2.at[3, theirs], ag_y_send.at[3], ag_y_recv.at[3], to_z(1)
        )

    def forward(index):
        ag_z_in(index).wait_recv()
        ag_z(index).start()
        ag_y(index).start()

    ag_z(0).start()

    mix_copies = []

    def turn(source, target, index):
        def turn_tile(tile, carry):
            at = pl.ds(pl.multiple_of(tile * span, 128), span)
            target[at, pl.ds(index * 2 * own, 2 * own)] = source[:, at].T
            return carry

        lax.fori_loop(0, z_size, turn_tile, 0)

    def chunk(index):
        if index:
            mix_copies[index - 1].wait()
        dy_loads[index].wait()
        rows_at = pl.ds(index * 2 * own, 2 * own)

        def up_tile(tile, carry):
            cols = pl.ds(pl.multiple_of(tile * TILE, TILE), TILE)
            gate = dot_nn(n2[index], w3[0, :, cols])
            up_proj = dot_nn(n2[index], w3[1, :, cols])
            grad_hidden = dot_nn(dy[...], w3[2, :, cols])
            act, slope = gelu_parts(gate)
            h3[0, rows_at, cols] = (grad_hidden * up_proj * slope).astype(jnp.bfloat16)
            h3[1, rows_at, cols] = (grad_hidden * act).astype(jnp.bfloat16)
            h3[2, rows_at, cols] = (act * up_proj).astype(jnp.bfloat16)
            return carry

        lax.fori_loop(0, units // TILE, up_tile, 0)

        def down_tile(tile, carry):
            at = pl.ds(pl.multiple_of(tile * span, 128), span)
            normed = matmul_nt(w3[0, at, :], h3[0, rows_at, :]) + matmul_nt(
                w3[1, at, :], h3[1, rows_at, :]
            )
            mixed = matmul_nt(w3[2, at, :], h3[2, rows_at, :])
            for half in range(2):
                cols = slice(half * own, (half + 1) * own)
                gn_part[index, half, at, :] = normed[:, cols].astype(jnp.bfloat16)
                mix_buf[half, at, :] = mixed[:, cols].astype(jnp.bfloat16)
            return carry

        lax.fori_loop(0, z_size, down_tile, 0)
        copy = pltpu.make_async_copy(mix_buf, mix_hbm.at[index], mix_sem.at[index])
        copy.start()
        mix_copies.append(copy)
        if index:
            rs_y(index).start()
        turn(n2.at[index], n2_t, index)
        turn(dy, dy_t, index)
        if index + 1 < z_size:
            dy_loads[index + 1].start()

    def rs_y(index):
        return remote(
            gn_part.at[index, 1 - me_y], gn_y.at[index], rs_y_send.at[index], rs_y_recv.at[index], to_y
        )

    def rs_z(index):
        return remote(
            gn_s.at[index - 1],
            gn_z.at[index - 1],
            rs_z_send.at[index],
            rs_z_recv.at[index - 1],
            to_z(1),
        )

    def rs_step(index):
        rs_y(index).wait_recv()
        slot = (index - 2) % z_size
        if index != 1:
            remote(
                gn_s.at[slot], gn_z.at[slot], rs_z_send.at[1], rs_z_recv.at[slot], to_z(1)
            ).wait_recv()

        def add_tile(tile, carry):
            at = pl.ds(pl.multiple_of(tile * TILE, TILE), TILE)
            total = gn_part[index, me_y, at, :].astype(jnp.float32) + gn_y[index, at, :].astype(
                jnp.float32
            )
            if index != 1:
                total = total + gn_z[slot, at, :].astype(jnp.float32)
            if index == 0:
                gm_ref[:, at] = total.T
            else:
                gn_s[index - 1, at, :] = total.astype(jnp.bfloat16)
            return carry

        lax.fori_loop(0, width // TILE, add_tile, 0)
        if index != 0:
            rs_z(index).start()


    def grads(step):
        at = pl.ds(pl.multiple_of(ahead(step) * span, 128), span)
        for kind, source in enumerate((n2_t, n2_t, dy_t)):

            def tile_body(tile, carry, kind=kind, source=source):
                cols = pl.ds(pl.multiple_of(tile * WIDE, WIDE), WIDE)
                w3[kind, at, cols] = dot_nn(source[at, :], h3[kind, :, cols]).astype(jnp.bfloat16)
                return carry

            lax.fori_loop(0, units // WIDE, tile_body, 0)
        for far in (1, 0):
            for kind in range(3):
                over_c(kind, step, far).start()

    def over_c(kind, step, far):
        x_at = 1 - me_x if far else me_x
        return remote(
            w3.at[kind, row_block(ahead(step), x_at, 1 - me_c)],
            c_in.at[kind, step, far],
            c_send.at[kind, step, far],
            c_recv.at[kind, step, far],
            to_c,
        )

    def over_x(kind):
        return remote(
            w3.at[kind, row_block(ahead(1), 1 - me_x, me_c)],
            x_in.at[kind],
            x_send.at[kind],
            x_recv.at[kind],
            to_x,
        )

    out_copies = []

    def keep(kind, step, far, block):
        copy = pltpu.make_async_copy(
            block, sums_hbm.at[kind, step, far], out_sem.at[kind, step, far]
        )
        copy.start()
        out_copies.append(copy)

    def core_sums(step):
        for far in (1, 0):
            for kind in range(3):
                over_c(kind, step, far).wait_recv()
                x_at = 1 - me_x if far else me_x
                block = w3.at[kind, row_block(ahead(step), x_at, me_c)]
                add_rows(block, [c_in.at[kind, step, far]], block, rows)
                if step != 1:
                    keep(kind, step, far, block)
                elif far:
                    over_x(kind).start()

    def first_sums():
        for kind in range(3):
            over_x(kind).wait_recv()
            block = w3.at[kind, row_block(ahead(1), me_x, me_c)]
            add_rows(block, [x_in.at[kind]], block, rows)
            keep(kind, 1, 0, block)

    own_load.wait()
    w_loads(lambda copy: copy.wait())

    @pl.when(outer)
    def _():
        w3[:, :, main:] = jnp.zeros((3, width, units - main), jnp.bfloat16)

    chunk(0)
    forward(1)
    forward(2)
    ag_y_in(1).wait_recv()
    chunk(1)
    ag_y_in(2).wait_recv()
    ag_last().start()
    chunk(2)
    rs_step(1)
    ag_z_in(3).wait_recv()
    ag_last().wait_recv()
    chunk(3)
    rs_y(0).start()
    rs_step(2)
    grads(1)
    grads(2)
    core_sums(1)
    rs_step(3)
    grads(3)
    core_sums(2)
    grads(0)
    core_sums(3)
    rs_step(0)
    core_sums(0)

    cot_load = pltpu.make_async_copy(
        dy_hbm.at[0, mine], dy.at[pl.ds(0, own)], load_sem.at[z_size + 3]
    )
    cot_load.start()
    cot_load.wait()
    mid_load.wait()

    def mid_rows(index, total):
        at = pl.ds(pl.multiple_of(index * 32, 32), 32)
        grad, gain_sum = norm_back(mid[at, :], gain_ref[1:2, :], gm_ref[at, :])
        grad = grad + dy[at, :].astype(jnp.float32)
        gm_ref[at, :] = grad
        dy[pl.ds(pl.multiple_of(own + index * 32, 32), 32), :] = grad.astype(jnp.bfloat16)
        return total + gain_sum

    gain_sum = lax.fori_loop(0, own // 32, mid_rows, jnp.zeros((1, width), jnp.float32))
    gm_save = pltpu.make_async_copy(dy.at[pl.ds(own, own)], gm_hbm, load_sem.at[z_size + 3])
    gm_save.start()
    for index in range(4):
        gain_part[index : index + 1, :] = jnp.zeros((1, span), jnp.float32)
        gain_part[4 + index : 5 + index, :] = gain_sum[:, index * span : (index + 1) * span]
    first_sums()
    gm_save.wait()

    for copy in mix_copies[3:] + out_copies:
        copy.wait()
    for index in range(z_size):
        if index in (1, 2):
            ag_y(index).wait_send()
        if index == 3:
            ag_last().wait_send()
        rs_y(index).wait_send()
        if index < z_size - 1:
            ag_z(index).wait_send()
        if index:
            rs_z(index).wait_send()
        for kind in range(3):
            over_c(kind, index, 0).wait_send()
            over_c(kind, index, 1).wait_send()
            if index == 1:
                over_x(kind).wait_send()


def ffn_call(gains, normed, grad_all, weights, mid, rows, main):
    z_size = lax.axis_size("z")
    pair, width = normed.shape
    units = weights.shape[2]
    own = pair // 2
    wide = lambda *lead: pltpu.VMEM((*lead, width), jnp.bfloat16)
    tall = lambda *lead: pltpu.VMEM((*lead, width, own), jnp.bfloat16)
    dma = lambda *lead: pltpu.SemaphoreType.DMA(lead)
    vmem = pl.BlockSpec(memory_space=pltpu.VMEM)
    hbm = pl.BlockSpec(memory_space=pl.ANY)
    return pl.pallas_call(
        functools.partial(ffn_kernel, z_size, main),
        out_shape=(
            jax.ShapeDtypeStruct((own, width), jnp.float32),
            jax.ShapeDtypeStruct((8, width // z_size), jnp.float32),
            jax.ShapeDtypeStruct((z_size, 2, width, own), jnp.bfloat16),
            jax.ShapeDtypeStruct((3, z_size, 2, rows, units), jnp.bfloat16),
            jax.ShapeDtypeStruct((own, width), jnp.bfloat16),
        ),
        in_specs=[vmem, hbm, hbm, hbm, hbm],
        out_specs=(vmem, vmem, hbm, hbm, hbm),
        scratch_shapes=[
            wide(z_size, pair),
            wide(pair),
            pltpu.VMEM(weights.shape, jnp.bfloat16),
            pltpu.VMEM((3, z_size * pair, units), jnp.bfloat16),
            pltpu.VMEM((width, z_size * pair), jnp.bfloat16),
            pltpu.VMEM((width, z_size * pair), jnp.bfloat16),
            tall(z_size, 2),
            tall(2),
            tall(z_size),
            tall(z_size - 1),
            tall(z_size - 1),
            pltpu.VMEM((3, z_size, 2, rows, units), jnp.bfloat16),
            pltpu.VMEM((3, rows, units), jnp.bfloat16),
            pltpu.VMEM((own, width), jnp.float32),
            dma(z_size + 5),
            dma(z_size),
            dma(z_size),
            dma(z_size),
            dma(z_size),
            dma(z_size),
            dma(z_size),
            dma(z_size),
            dma(z_size),
            dma(z_size),
            dma(3, z_size, 2),
            dma(3, z_size, 2),
            dma(3),
            dma(3),
            dma(3, z_size, 2),
        ],
        compiler_params=pltpu.CompilerParams(
            collective_id=0, has_side_effects=True, vmem_limit_bytes=VMEM_BYTES
        ),
        cost_estimate=pl.CostEstimate(
            flops=18 * z_size * pair * width * units,
            bytes_accessed=4 * weights.size + 12 * z_size * pair * width,
            transcendentals=z_size * pair * units,
        ),
    )(gains, normed, grad_all, weights, mid)


def spin(values, table):
    first = values[:, : values.shape[1] // 2]
    turned = first * table[0] + pltpu.roll(first, first.shape[1] // 2, 1) * table[1]
    return jnp.concatenate([turned, values[:, values.shape[1] // 2 :]], axis=1)


def spin_back(values, table):
    first = values[:, : values.shape[1] // 2]
    turned = first * table[0] - pltpu.roll(first, first.shape[1] // 2, 1) * table[1]
    return jnp.concatenate([turned, values[:, values.shape[1] // 2 :]], axis=1)


def head_probs(rotated, keys, allowed):
    scores = jnp.where(allowed > 0.5, matmul_nt(rotated, keys), masked_score)
    weights = jnp.exp(scores - jnp.max(scores, axis=-1, keepdims=True))
    return weights / jnp.sum(weights, axis=-1, keepdims=True)


def ragged_split(columns, parts):
    main = columns // parts // 128 * 128
    return main, main + 128


def pre_kernel(
    z_size,
    tok_ref,
    wkv_ref,
    gains_ref,
    table_ref,
    seg_ref,
    cot_hbm,
    wq_hbm,
    wo_hbm,
    wg_hbm,
    wu_hbm,
    wd_hbm,
    n1_ref,
    rot_ref,
    key_ref,
    val_ref,
    att_ref,
    mid_ref,
    n2_ref,
    gain_ref,
    allow_ref,
    kv_out,
    wq_out,
    wo_out,
    w3_out,
    dy_out,
    kv_w,
    q_w,
    o_w,
    tok,
    part,
    part_y,
    query,
    y_send,
    y_recv,
    ky_send,
    ky_recv,
    az_send,
    az_recv,
    ax_send,
    ax_recv,
    ac_send,
    ac_recv,
    fz_send,
    fz_recv,
    fx_send,
    fx_recv,
    fc_send,
    fc_recv,
    dz_send,
    dz_recv,
    dy_send,
    dy_recv,
    local_sem,
):
    me_z, me_x = lax.axis_index("z"), lax.axis_index("x")
    me_c, me_y = lax.axis_index("c"), lax.axis_index("mp")
    own, width = tok_ref.shape
    rows = wq_hbm.shape[0]
    half_rows = wkv_ref.shape[0]
    head = key_ref.shape[1]
    main, units = ragged_split(wg_hbm.shape[1], z_size)
    to_y, to_x, to_c = {"mp": 1 - me_y}, {"x": 1 - me_x}, {"c": 1 - me_c}

    def to_z(step):
        return {"z": lax.rem(me_z + step, z_size)}

    def from_z(step):
        return lax.rem(me_z - step + z_size, z_size)

    def row_block(step, x_at, c_at):
        start = ((from_z(step) * 2 + x_at) * 2 + c_at) * rows
        return pl.ds(pl.multiple_of(start, rows), rows)

    mine = pl.ds(pl.multiple_of(me_y * own, own), own)
    theirs = pl.ds(pl.multiple_of((1 - me_y) * own, own), own)
    bufs = (kv_w, q_w, o_w)
    inputs = (None, wq_hbm, wo_hbm)

    locals_ = []

    def local(src, dst):
        copy = pltpu.make_async_copy(src, dst, local_sem.at[len(locals_)])
        copy.start()
        locals_.append(copy)
        return copy

    here = row_block(0, me_x, me_c)
    own_q = local(wq_hbm, q_w.at[here])
    own_o = local(wo_hbm, o_w.at[here])
    ffn_in = (wg_hbm, wu_hbm, wd_hbm)

    def body_of(target):
        return pl.ds(pl.multiple_of(target * main, 128), main), pl.ds(0, main)

    def tail_of(target):
        start = z_size * main + lax.rem(target + 1, 2) * 128
        return pl.ds(pl.multiple_of(start, 128), 128), pl.ds(main, 128)

    def is_inner(at):
        return (at > 0) & (at < z_size - 1)

    own_f = []
    for kind in range(3):
        src, dst = body_of(me_z)
        own_f.append(local(ffn_in[kind].at[:, src], w3_out.at[kind, here, dst]))

    def own_tail(kind):
        src, dst = tail_of(me_z)
        return pltpu.make_async_copy(
            ffn_in[kind].at[:, src], w3_out.at[kind, here, dst], local_sem.at[12 + kind]
        )

    @pl.when(is_inner(me_z))
    def _():
        for kind in range(3):
            own_tail(kind).start()
    own_d = local(cot_hbm, dy_out.at[0, mine])

    kv_own = pl.ds(pl.multiple_of(here.start + me_y * half_rows, half_rows), half_rows)
    spread = jnp.concatenate([gains_ref[...], jnp.zeros((120, 128), jnp.float32)], axis=0).T
    kv_w[kv_own, : 2 * head] = wkv_ref[...]
    kv_w[kv_own, 2 * head :] = spread[:half_rows, :].astype(jnp.bfloat16)

    barrier = pltpu.get_barrier_semaphore()
    peers = [to_y, to_x, to_c] + [to_z(step) for step in range(1, z_size)]
    for where in peers:
        pl.semaphore_signal(barrier, inc=1, device_id=where, device_id_type=MESH_ID)
    pl.semaphore_wait(barrier, len(peers))

    tok_y = remote(tok_ref, tok.at[mine], y_send.at[1], y_recv.at[1], to_y)
    tok_y_in = remote(tok_ref, tok.at[theirs], y_send.at[1], y_recv.at[1], to_y)
    part_out = remote(part.at[theirs], part_y, y_send.at[2], y_recv.at[2], to_y)
    n2_y = remote(n2_ref.at[mine], n2_ref.at[mine], y_send.at[3], y_recv.at[3], to_y)
    n2_y_in = remote(n2_ref.at[theirs], n2_ref.at[theirs], y_send.at[3], y_recv.at[3], to_y)

    def block_of(kind, step, x_at):
        if kind:
            return row_block(step, x_at, me_c)
        return kv_rows(step, x_at, me_y)

    def kv_rows(step, x_at, y_at):
        start = row_block(step, x_at, me_c).start + y_at * half_rows
        return pl.ds(pl.multiple_of(start, half_rows), half_rows)

    def kv_y(step, far):
        x_at = 1 - me_x if far else me_x
        block = kv_w.at[kv_rows(step, x_at, me_y)]
        slot = step + z_size * far
        return remote(block, block, ky_send.at[slot], ky_recv.at[slot], to_y)

    def kv_y_in(step, far):
        x_at = 1 - me_x if far else me_x
        block = kv_w.at[kv_rows(step, x_at, 1 - me_y)]
        slot = step + z_size * far
        return remote(block, block, ky_send.at[slot], ky_recv.at[slot], to_y)

    def source(kind, step):
        if isinstance(step, int) and step == 0 and kind:
            return inputs[kind]
        return bufs[kind].at[block_of(kind, step, me_x)]

    first_z, last_z = (z_size - 1 - me_z) // (z_size - 1), me_z // (z_size - 1)
    inner = first_z + last_z == 0
    order = (0, 1 + 2 * first_z, 3 - first_z - last_z, 2 - first_z + last_z)
    hops = (
        None,
        (lax.rem(me_z + 1, z_size), 2),
        (lax.rem(me_z + z_size - 1, z_size), 2),
        (lax.rem(3 * (me_z + 3), z_size), lax.rem(2 * me_z + 3, z_size)),
    )

    def a_z_own(kind, right):
        return remote(
            source(kind, 0),
            bufs[kind].at[block_of(kind, 0, me_x)],
            az_send.at[kind, right],
            az_recv.at[kind, 1 if right else z_size - 1],
            to_z(1 if right else z_size - 1),
        )

    def a_z_start(kind):
        @pl.when(last_z == 0)
        def _():
            a_z_own(kind, 1).start()

        @pl.when(first_z == 0)
        def _():
            a_z_own(kind, 0).start()

    def a_z(kind, index):
        target, slot = hops[index]
        block = bufs[kind].at[block_of(kind, order[index], me_x)]
        return remote(
            block, block, az_send.at[kind, 1 + index], az_recv.at[kind, slot], {"z": target}
        )

    def a_z_next(kind, index):
        @pl.when(inner)
        def _():
            a_z(kind, index).start()

    def a_z_done(kind):
        @pl.when(last_z == 0)
        def _():
            a_z_own(kind, 1).wait_send()

        @pl.when(first_z == 0)
        def _():
            a_z_own(kind, 0).wait_send()

        @pl.when(inner)
        def _():
            for index in range(1, z_size):
                a_z(kind, index).wait_send()

    def a_z_in(kind, step):
        block = bufs[kind].at[block_of(kind, step, me_x)]
        return remote(block, block, az_send.at[kind, 0], az_recv.at[kind, step], to_z(1))

    def a_x(kind, step):
        return remote(
            source(kind, step),
            bufs[kind].at[block_of(kind, step, me_x)],
            ax_send.at[kind, step],
            ax_recv.at[kind, step],
            to_x,
        )

    def a_x_in(kind, step):
        block = bufs[kind].at[block_of(kind, step, 1 - me_x)]
        return remote(block, block, ax_send.at[kind, step], ax_recv.at[kind, step], to_x)

    def a_c(kind, step, far):
        x_at = 1 - me_x if far else me_x
        block = bufs[kind].at[row_block(step, x_at, me_c)]
        src = source(kind, step) if kind and not far else block
        slot = step + z_size * far
        return remote(src, block, ac_send.at[kind, slot], ac_recv.at[kind, slot], to_c)

    def a_c_in(kind, step, far):
        x_at = 1 - me_x if far else me_x
        block = bufs[kind].at[row_block(step, x_at, 1 - me_c)]
        slot = step + z_size * far
        return remote(block, block, ac_send.at[kind, slot], ac_recv.at[kind, slot], to_c)

    def f_z(kind, step, act):
        target = lax.rem(me_z + step, z_size)

        def piece(index, src, dst):
            return remote(
                ffn_in[kind].at[:, src],
                w3_out.at[kind, here, dst],
                fz_send.at[kind, step, index],
                fz_recv.at[kind, step, index],
                to_z(step),
            )

        act(piece(0, *body_of(target)))

        @pl.when(is_inner(target))
        def _():
            act(piece(1, *tail_of(target)))

    def f_z_wait(kind, step):
        block = row_block(step, me_x, me_c)

        def piece(index, dst):
            part = w3_out.at[kind, block, dst]
            return remote(
                part, part, fz_send.at[kind, step, index], fz_recv.at[kind, step, index], to_z(step)
            )

        piece(0, pl.ds(0, main)).wait_recv()

        @pl.when(inner)
        def _():
            piece(1, pl.ds(main, 128)).wait_recv()

    def f_x(kind, step, x_at, act):
        for case, columns in ((inner, units), (first_z + last_z > 0, main)):

            @pl.when(case)
            def _(columns=columns):
                block = w3_out.at[kind, row_block(step, x_at, me_c), pl.ds(0, columns)]
                act(remote(block, block, fx_send.at[kind, step], fx_recv.at[kind, step], to_x))

    def f_x_start(kind, step):
        f_x(kind, step, me_x, lambda copy: copy.start())

    def f_x_wait(kind, step):
        f_x(kind, step, 1 - me_x, lambda copy: copy.wait_recv())

    def f_x_done(kind, step):
        f_x(kind, step, me_x, lambda copy: copy.wait_send())

    def f_c(kind, step, far):
        block = w3_out.at[kind, row_block(step, 1 - me_x if far else me_x, me_c)]
        slot = step + z_size * far
        return remote(block, block, fc_send.at[kind, slot], fc_recv.at[kind, slot], to_c)

    def f_c_in(kind, step, far):
        block = w3_out.at[kind, row_block(step, 1 - me_x if far else me_x, 1 - me_c)]
        slot = step + z_size * far
        return remote(block, block, fc_send.at[kind, slot], fc_recv.at[kind, slot], to_c)

    def d_source(step):
        return cot_hbm if isinstance(step, int) else dy_out.at[step, mine]

    def d_z_own(right):
        slot = 1 if right else z_size - 1
        return remote(
            cot_hbm, dy_out.at[slot, mine], dz_send.at[right], dz_recv.at[slot], to_z(slot)
        )

    def d_z(index):
        target, slot = hops[index]
        return remote(
            dy_out.at[order[index], mine],
            dy_out.at[slot, mine],
            dz_send.at[1 + index],
            dz_recv.at[slot],
            {"z": target},
        )

    def d_z_done():
        @pl.when(last_z == 0)
        def _():
            d_z_own(1).wait_send()

        @pl.when(first_z == 0)
        def _():
            d_z_own(0).wait_send()

        @pl.when(inner)
        def _():
            for index in range(1, z_size):
                d_z(index).wait_send()

    def d_z_in(step):
        block = dy_out.at[step, mine]
        return remote(block, block, dz_send.at[0], dz_recv.at[step], to_z(1))

    def d_y(step):
        return remote(
            d_source(step), dy_out.at[step, mine], dy_send.at[step], dy_recv.at[step], to_y
        )

    def d_y_in(step):
        block = dy_out.at[step, theirs]
        return remote(block, block, dy_send.at[step], dy_recv.at[step], to_y)

    for kind in (1, 0, 2):
        a_z_start(kind)
        a_x(kind, 0).start()
    kv_y(0, 0).start()
    tok_y.start()
    for kind in (1, 2):
        a_c(kind, 0, 0).start()

    for at_end, away in ((first_z, 1), (last_z, z_size - 1)):

        @pl.when(at_end > 0)
        def _(away=away):
            d_z_own(1 if away == 1 else 0).start()
            for kind in range(3):
                f_z(kind, away, lambda copy: copy.start())

    tok[mine, :] = tok_ref[...]
    seq = 2 * own
    query_at = lax.broadcasted_iota(jnp.int32, (seq, seq), 0)
    key_at = lax.broadcasted_iota(jnp.int32, (seq, seq), 1)
    same = seg_ref[...].T[:, :1] == seg_ref[:1, :]
    allowed = same & (key_at <= query_at) & (query_at - key_at < WINDOW)
    allow_ref[...] = jnp.where(allowed, 1.0, 0.0)
    d_y(0).start()

    def from_x(index):
        step = order[index]
        for kind in (1, 0, 2):
            a_x_in(kind, step).wait_recv()
            if kind:
                a_c(kind, step, 1).start()
            else:
                kv_y(step, 1).start()

    def from_y(index):
        step = order[index]
        for far in range(2):
            kv_y_in(step, far).wait_recv()
            a_c(0, step, far).start()

    def pass_cotangent(index):
        d_z_in(order[index]).wait_recv()

        @pl.when(inner)
        def _():
            d_z(index).start()

        d_y(order[index]).start()

    outer = first_z + last_z > 0

    def only(case, *acts):
        @pl.when(case)
        def _():
            for act, *args in acts:
                act(*args)

    def send_ffn(*ways):
        for kind in range(3):
            for away in ways:
                f_z(kind, away, lambda copy: copy.start())

    def own_cotangent():
        d_z_own(1).start()
        d_z_own(0).start()

    for index in range(1, z_size):
        step = order[index]
        for kind in (1, 0, 2):
            a_z_in(kind, step).wait_recv()
            a_z_next(kind, index)
            a_x(kind, step).start()
            if kind:
                a_c(kind, step, 0).start()
            else:
                kv_y(step, 0).start()
        if index == z_size - 1:
            only(inner, (own_cotangent,), (pass_cotangent, 1))
            only(first_z > 0, (send_ffn, 2, 3))
            only(last_z > 0, (send_ffn, 2, 1))
        if index >= 2:
            from_x(index - 2)
            from_y(index - 2)

    def hand_on(kind, index):
        step = order[index]
        f_z_wait(kind, step)
        f_x_start(kind, step)
        f_c(kind, step, 0).start()

    def cross(kind, index):
        f_x_wait(kind, order[index])
        f_c(kind, order[index], 1).start()

    from_x(z_size - 2)
    only(inner, (pass_cotangent, 2))
    from_y(z_size - 2)
    only(inner, (pass_cotangent, 3), (send_ffn, 1, 3, 2))
    for copy in own_f:
        copy.wait()

    @pl.when(inner)
    def _():
        for kind in range(3):
            own_tail(kind).wait()

    for kind in range(3):
        f_x_start(kind, 0)
        f_c(kind, 0, 0).start()
    from_x(z_size - 1)
    from_y(z_size - 1)
    only(outer, (pass_cotangent, 1))
    tok_y_in.wait_recv()
    own_q.wait()
    own_o.wait()
    for kind in (0, 1):
        for step in range(z_size):
            for far in range(2):
                a_c_in(kind, step, far).wait_recv()

    gains = kv_w[:, 2 * head :].astype(jnp.float32).T[:8, :]
    gain_ref[...] = gains

    def norm_rows(index, carry):
        at = pl.ds(pl.multiple_of(index * 32, 32), 32)
        values = tok[at, :].astype(jnp.float32)
        scale = lax.rsqrt(jnp.mean(values * values, axis=-1, keepdims=True) + epsilon)
        n1_ref[at, :] = (values * scale * gain_ref[0:1, :]).astype(jnp.bfloat16)
        return carry

    lax.fori_loop(0, 2 * own // 32, norm_rows, 0)
    only(inner, (hand_on, 0, 1))
    table = (table_ref[0], table_ref[1])
    key_ref[...] = spin(dot_nn(n1_ref[...], kv_w[:, :head]), table).astype(jnp.bfloat16)
    val_ref[...] = dot_nn(n1_ref[...], kv_w[:, head : 2 * head]).astype(jnp.bfloat16)
    head_scale = head ** (-0.5)
    heads = att_ref.shape[1] // head

    half_cols = att_ref.shape[1] // 2
    for index in range(2):
        cols = pl.ds(index * half_cols, half_cols)
        query[:, cols] = dot_nn(n1_ref[...], q_w[:, cols])

    def attend(index):
        cols = pl.ds(index * head, head)
        rotated = (spin(query[:, cols], table) * head_scale).astype(jnp.bfloat16)
        rot_ref[:, cols] = rotated
        probs = head_probs(rotated, key_ref[...], allow_ref[...]).astype(jnp.bfloat16)
        att_ref[:, cols] = dot_nn(probs, val_ref[...]).astype(jnp.bfloat16)

    tasks = [
        lambda: only(inner, (hand_on, 0, 2)),
        lambda: (cross(0, 0), only(outer, (pass_cotangent, 2))),
        lambda: (cross(1, 0), only(inner, (hand_on, 0, 3))),
        lambda: only(inner, (hand_on, 1, 1)),
        lambda: (cross(2, 0), only(outer, (pass_cotangent, 3))),
    ]
    for index in range(heads):
        attend(index)
        if index < len(tasks):
            tasks[index]()
    for step in range(z_size):
        for far in range(2):
            a_c_in(2, step, far).wait_recv()
    saves = [
        local(kv_w, kv_out),
        local(q_w, wq_out),
        local(o_w, wo_out),
    ]
    span = width // 4

    def project(index, carry):
        cols = pl.ds(pl.multiple_of(index * span, span), span)
        part[:, cols] = matmul_nt(att_ref[...], o_w[cols, :]).astype(jnp.bfloat16)
        return carry

    lax.fori_loop(0, 4, project, 0)
    part_out.start()
    only(outer, (hand_on, 0, 1), (hand_on, 0, 2))
    only(inner, (hand_on, 1, 2), (cross, 0, 1))
    part_out.wait_recv()

    def middle(index, carry):
        at = pl.ds(pl.multiple_of(index * 32, 32), 32)
        there = pl.ds(pl.multiple_of(me_y * own + index * 32, 32), 32)
        values = (
            tok_ref[at, :].astype(jnp.float32)
            + part[there, :].astype(jnp.float32)
            + part_y[at, :].astype(jnp.float32)
        )
        mid_ref[at, :] = values
        scale = lax.rsqrt(jnp.mean(values * values, axis=-1, keepdims=True) + epsilon)
        n2_ref[there, :] = (values * scale * gain_ref[1:2, :]).astype(jnp.bfloat16)
        return carry

    lax.fori_loop(0, own // 32, middle, 0)
    n2_y.start()
    only(outer, (hand_on, 0, 3), (cross, 0, 1), (hand_on, 1, 1))
    only(inner, (hand_on, 1, 3))
    cross(0, 2)
    hand_on(2, 1)
    only(outer, (hand_on, 1, 2), (hand_on, 1, 3))
    cross(0, 3)
    hand_on(2, 2)
    cross(1, 1)
    hand_on(2, 3)
    cross(1, 2)
    cross(1, 3)
    for index in (1, 2, 3):
        cross(2, index)
    for kind in range(3):
        for step in range(z_size):
            for far in range(2):
                f_c_in(kind, step, far).wait_recv()
    for step in range(z_size):
        d_y_in(step).wait_recv()
    n2_y_in.wait_recv()

    for kind in range(3):
        a_z_done(kind)
    d_z_done()
    tok_y.wait_send()
    part_out.wait_send()
    n2_y.wait_send()
    own_d.wait()
    for copy in saves:
        copy.wait()
    for step in range(z_size):
        d_y(step).wait_send()
        for far in range(2):
            kv_y(step, far).wait_send()
        for kind in range(3):
            if step:
                f_z(kind, step, lambda copy: copy.wait_send())
            a_x(kind, step).wait_send()
            f_x_done(kind, step)
            for far in range(2):
                a_c(kind, step, far).wait_send()
                f_c(kind, step, far).wait_send()


def pre_call(tokens, w_kv, gains, table, segments, cotangent, w_query, w_out, ffn):
    z_size = lax.axis_size("z")
    own, width = tokens.shape
    seq = 2 * own
    rows, cols = w_query.shape
    head = table.shape[2] * 2
    units = ragged_split(ffn[0].shape[1], z_size)[1]
    low = lambda *dims: jax.ShapeDtypeStruct(dims, jnp.bfloat16)
    full = lambda *dims: jax.ShapeDtypeStruct(dims, jnp.float32)
    dma = lambda *lead: pltpu.SemaphoreType.DMA(lead)
    vmem = pl.BlockSpec(memory_space=pltpu.VMEM)
    hbm = pl.BlockSpec(memory_space=pl.ANY)
    wide = lambda *lead: pltpu.VMEM((*lead, width), jnp.bfloat16)
    return pl.pallas_call(
        functools.partial(pre_kernel, z_size),
        out_shape=(
            low(seq, width),
            low(seq, cols),
            low(seq, head),
            low(seq, head),
            low(seq, cols),
            full(own, width),
            low(seq, width),
            full(8, width),
            full(seq, seq),
            low(width, 2 * head + 128),
            low(width, cols),
            low(width, cols),
            low(3, width, units),
            low(z_size, seq, width),
        ),
        in_specs=[vmem] * 5 + [hbm] * 6,
        out_specs=(vmem,) * 9 + (hbm,) * 5,
        scratch_shapes=[
            pltpu.VMEM((width, 2 * head + 128), jnp.bfloat16),
            pltpu.VMEM((width, cols), jnp.bfloat16),
            pltpu.VMEM((width, cols), jnp.bfloat16),
            wide(seq),
            wide(seq),
            wide(own),
            pltpu.VMEM((seq, cols), jnp.float32),
            dma(4),
            dma(4),
            dma(2 * z_size),
            dma(2 * z_size),
            dma(3, z_size + 1),
            dma(3, z_size),
            dma(3, z_size),
            dma(3, z_size),
            dma(3, 2 * z_size),
            dma(3, 2 * z_size),
            dma(3, z_size, 2),
            dma(3, z_size, 2),
            dma(3, z_size),
            dma(3, z_size),
            dma(3, 2 * z_size),
            dma(3, 2 * z_size),
            dma(z_size + 1),
            dma(z_size),
            dma(z_size),
            dma(z_size),
            dma(16),
        ],
        compiler_params=pltpu.CompilerParams(
            collective_id=1, has_side_effects=True, vmem_limit_bytes=VMEM_BYTES
        ),
        cost_estimate=pl.CostEstimate(
            flops=8 * seq * width * cols,
            bytes_accessed=8 * width * (cols + units),
            transcendentals=seq * seq * cols // head,
        ),
    )(tokens, w_kv, gains, table, segments, cotangent, w_query, w_out, *ffn)


def post_kernel(
    z_size,
    main,
    tok_ref,
    gain_ref,
    gain_part_ref,
    n1_ref,
    rot_ref,
    key_ref,
    val_ref,
    att_ref,
    table_ref,
    allow_ref,
    kv_hbm,
    wq_hbm,
    wo_hbm,
    mix_hbm,
    gmf_hbm,
    gmb_hbm,
    mid_hbm,
    sums_hbm,
    mixed_ref,
    tgrad_ref,
    gsum_ref,
    kvg_ref,
    qg_ref,
    og_ref,
    ffn_out,
    kv_w,
    q_w,
    o_w,
    o_part,
    gm,
    gm_f,
    gq,
    gkv,
    kv_sum,
    back_y,
    mix_y,
    mix_z,
    mix_s,
    o_c,
    o_x,
    o_z,
    q_c,
    q_x,
    q_z,
    kv_y,
    kv_c,
    kv_x,
    kv_z,
    gain_own,
    gain_in,
    ffn_in,
    ffn_own,
    load_sem,
    own_sem,
    fx_send,
    fx_recv,
    fz_send,
    fz_recv,
    y_send,
    y_recv,
    my_send,
    my_recv,
    mz_send,
    mz_recv,
    wc_send,
    wc_recv,
    wx_send,
    wx_recv,
    wz_send,
    wz_recv,
    kc_send,
    kc_recv,
    kz_send,
    kz_recv,
    g_send,
    g_recv,
):
    me_z, me_x = lax.axis_index("z"), lax.axis_index("x")
    me_c, me_y = lax.axis_index("c"), lax.axis_index("mp")
    own, width = tok_ref.shape
    seq = 2 * own
    head = key_ref.shape[1]
    cols_here = att_ref.shape[1]
    heads = cols_here // head
    rows = qg_ref.shape[0]
    span = width // z_size
    mine = pl.ds(pl.multiple_of(me_y * own, own), own)
    theirs = pl.ds(pl.multiple_of((1 - me_y) * own, own), own)
    to_y, to_x, to_c = {"mp": 1 - me_y}, {"x": 1 - me_x}, {"c": 1 - me_c}
    head_scale = head ** (-0.5)

    def behind(step):
        return lax.rem(me_z - step + z_size, z_size)

    def to_z(step):
        return {"z": lax.rem(me_z + step, z_size)}

    def row_block(step, x_at, c_at):
        start = ((behind(step) * 2 + x_at) * 2 + c_at) * rows
        return pl.ds(pl.multiple_of(start, rows), rows)

    loads = [
        pltpu.make_async_copy(wo_hbm, o_w, load_sem.at[0]),
        pltpu.make_async_copy(wq_hbm, q_w, load_sem.at[1]),
        pltpu.make_async_copy(
            kv_hbm.at[:, :, :, :, :, pl.ds(0, 2 * head)], kv_w, load_sem.at[2]
        ),
    ]
    for step in range(z_size):
        loads.append(
            pltpu.make_async_copy(mix_hbm.at[step, me_y], mix_s.at[step], load_sem.at[3 + step])
        )
    loads.append(pltpu.make_async_copy(gmf_hbm, gm_f, load_sem.at[3 + z_size]))
    loads.append(pltpu.make_async_copy(gmb_hbm, gm.at[mine], load_sem.at[4 + z_size]))
    mid_load = pltpu.make_async_copy(mid_hbm, gm_f, load_sem.at[5 + z_size])
    for load in loads:
        load.start()

    barrier = pltpu.get_barrier_semaphore()
    peers = [to_y, to_x, to_c] + [to_z(step) for step in range(1, z_size)]
    for where in peers:
        pl.semaphore_signal(barrier, inc=1, device_id=where, device_id_type=MESH_ID)
    pl.semaphore_wait(barrier, len(peers))

    tasks = [(step, kind) for step in (2, 3) for kind in range(3)]

    def f_x(index):
        step, kind = tasks[index]
        return remote(
            sums_hbm.at[kind, step, 1],
            ffn_in.at[index],
            fx_send.at[index],
            fx_recv.at[index],
            to_x,
        )

    def f_own(index):
        step, kind = tasks[index]
        return pltpu.make_async_copy(
            sums_hbm.at[kind, step, 0], ffn_own.at[index % 2], own_sem.at[index % 2]
        )

    def f_z(step, kind, source_z, act):
        for case, columns in (
            ((source_z > 0) & (source_z < z_size - 1), ffn_out.shape[3]),
            ((source_z == 0) | (source_z == z_size - 1), main),
        ):

            @pl.when(case)
            def _(columns=columns):
                cols = pl.ds(0, columns)
                if step == 1:
                    src = sums_hbm.at[kind, 1, 0, :, cols]
                else:
                    src = ffn_in.at[tasks.index((step, kind)), :, cols]
                act(
                    remote(
                        src,
                        ffn_out.at[kind, step, :, cols],
                        fz_send.at[kind, step],
                        fz_recv.at[kind, step],
                        to_z(step),
                    )
                )

    def tick(index):
        step, kind = tasks[index]
        f_x(index).wait_recv()
        f_own(index).wait()
        block = ffn_in.at[index]
        add_rows(block, [ffn_own.at[index % 2]], block, rows)
        if index + 2 < len(tasks):
            f_own(index + 2).start()
        f_z(step, kind, me_z, lambda copy: copy.start())

    def f_x_own(kind):
        return remote(
            sums_hbm.at[kind, 0, 1],
            ffn_out.at[kind, 0],
            fx_send.at[len(tasks) + kind],
            fx_recv.at[len(tasks) + kind],
            to_x,
        )

    f_own(0).start()
    f_own(1).start()
    for index in range(len(tasks)):
        f_x(index).start()
    for kind in range(3):
        f_z(1, kind, me_z, lambda copy: copy.start())

    gm_y = remote(gmb_hbm, gm.at[mine], y_send.at[0], y_recv.at[0], to_y)
    gm_y_in = remote(gm.at[theirs], gm.at[theirs], y_send.at[0], y_recv.at[0], to_y)
    gm_y.start()

    first_z, last_z = (z_size - 1 - me_z) // (z_size - 1), me_z // (z_size - 1)
    inner = first_z + last_z == 0
    order = (
        0,
        1 + (me_z + 1) // 2,
        2 + (2 * me_z - 3) * (1 - first_z - last_z),
        3 - 2 * (me_z // 2),
    )
    right = (None, 1 - me_z // 2, (3 - me_z) * (2 - me_z) // 6 + me_z // 2 * (1 - last_z), 1 - me_z // 2)

    def hop_slot(index):
        step, way = order[index], right[index]
        return way * lax.rem(step + 1, z_size) + (1 - way) * (step - 1 + 4 * ((3 - step) // 2))

    def hop_target(index):
        return {"z": me_z + 2 * right[index] - 1}

    def mix_over_y(step):
        return remote(
            mix_hbm.at[step, 1 - me_y], mix_y.at[step], my_send.at[step], my_recv.at[step], to_y
        )

    def mix_over_z(index):
        slot = hop_slot(index)
        return remote(
            mix_s.at[order[index]],
            mix_z.at[slot],
            mz_send.at[index],
            mz_recv.at[slot],
            hop_target(index),
        )

    def mix_z_in(slot):
        return remote(mix_z.at[slot], mix_z.at[slot], mz_send.at[1], mz_recv.at[slot], to_z(1))

    def mix_add(step, others, last):
        def add_tile(tile, carry):
            at = pl.ds(pl.multiple_of(tile * TILE, TILE), TILE)
            total = mix_s[step, at, :].astype(jnp.float32)
            for other in others:
                total = total + other[at, :].astype(jnp.float32)
            if last:
                mixed_ref[:, at] = (gm_f[:, at] + total.T).astype(jnp.bfloat16)
            else:
                mix_s[step, at, :] = total.astype(jnp.bfloat16)
            return carry

        lax.fori_loop(0, width // TILE, add_tile, 0)

    def mix_step(index):
        step = order[index]
        mix_over_y(step).wait_recv()
        from_y = mix_y.at[step]
        if index:

            @pl.when(inner)
            def _():
                mix_z_in(step).wait_recv()
                mix_add(step, [from_y, mix_z.at[step]], False)

            @pl.when(first_z + last_z > 0)
            def _():
                mix_add(step, [from_y], False)

            mix_over_z(index).start()
        else:
            mid_load.wait()

            @pl.when(first_z == 0)
            def _():
                mix_z_in(0).wait_recv()

            @pl.when(last_z == 0)
            def _():
                mix_z_in(z_size).wait_recv()

            @pl.when(inner)
            def _():
                mix_add(0, [from_y, mix_z.at[0], mix_z.at[z_size]], True)

            @pl.when(first_z > 0)
            def _():
                mix_add(0, [from_y, mix_z.at[z_size]], True)

            @pl.when(last_z > 0)
            def _():
                mix_add(0, [from_y, mix_z.at[0]], True)

    for index in (1, 2, 3, 0):
        mix_over_y(order[index]).start()

    kinds = ((o_part, o_c, o_x, o_z, og_ref), (o_w, q_c, q_x, q_z, qg_ref))

    def w_c(kind, step, far):
        x_at = 1 - me_x if far else me_x
        return remote(
            kinds[kind][0].at[row_block(step, x_at, 1 - me_c)],
            kinds[kind][1].at[step, far],
            wc_send.at[kind, step, far],
            wc_recv.at[kind, step, far],
            to_c,
        )

    def w_x(kind, step):
        return remote(
            kinds[kind][0].at[row_block(step, 1 - me_x, me_c)],
            kinds[kind][2].at[step],
            wx_send.at[kind, step],
            wx_recv.at[kind, step],
            to_x,
        )

    def w_z(kind, index):
        step, slot = order[index], hop_slot(index)
        return remote(
            kinds[kind][0].at[row_block(step, me_x, me_c)],
            kinds[kind][3].at[slot],
            wz_send.at[kind, index],
            wz_recv.at[kind, slot],
            hop_target(index),
        )

    def w_z_in(kind, slot):
        block = kinds[kind][3].at[slot]
        return remote(block, block, wz_send.at[kind, 1], wz_recv.at[kind, slot], to_z(1))

    def w_x_stage(kind, index):
        step = order[index]
        w_c(kind, step, 1).wait_recv()
        block = kinds[kind][0].at[row_block(step, 1 - me_x, me_c)]
        add_rows(block, [kinds[kind][1].at[step, 1]], block, rows)
        w_x(kind, step).start()

    def w_z_stage(kind, index):
        part, from_c, from_x, from_z, result = kinds[kind]
        step = order[index]
        w_c(kind, step, 0).wait_recv()
        w_x(kind, step).wait_recv()
        block = part.at[row_block(step, me_x, me_c)]
        others = [from_c.at[step, 0], from_x.at[step]]
        if index:

            @pl.when(inner)
            def _():
                w_z_in(kind, step).wait_recv()
                add_rows(block, [*others, from_z.at[step]], block, rows)

            @pl.when(first_z + last_z > 0)
            def _():
                add_rows(block, others, block, rows)

            w_z(kind, index).start()
        else:

            @pl.when(first_z == 0)
            def _():
                w_z_in(kind, 0).wait_recv()

            @pl.when(last_z == 0)
            def _():
                w_z_in(kind, z_size).wait_recv()

            @pl.when(inner)
            def _():
                add_rows(block, [*others, from_z.at[0], from_z.at[z_size]], result, rows)

            @pl.when(first_z > 0)
            def _():
                add_rows(block, [*others, from_z.at[z_size]], result, rows)

            @pl.when(last_z > 0)
            def _():
                add_rows(block, [*others, from_z.at[0]], result, rows)

    def w_product(kind, index, left, values):
        step = order[index]
        at = pl.ds(pl.multiple_of(behind(step) * span, 128), span)
        turned = left[:, at].T

        def tile_body(tile, carry):
            cols = pl.ds(pl.multiple_of(tile * TILE, TILE), TILE)
            kinds[kind][0][at, cols] = dot_nn(turned, values[:, cols]).astype(jnp.bfloat16)
            return carry

        lax.fori_loop(0, cols_here // TILE, tile_body, 0)
        for far in (1, 0):
            w_c(kind, step, far).start()

    outer = first_z + last_z > 0

    def if_outer(act, *args):
        @pl.when(outer)
        def _():
            act(*args)

    def if_inner(act, *args):
        @pl.when(inner)
        def _():
            act(*args)

    tick(0)
    tick(1)
    loads[-1].wait()
    gm_y_in.wait_recv()
    w_product(0, 1, gm, att_ref)
    w_product(0, 2, gm, att_ref)
    w_x_stage(0, 1)
    tick(2)
    w_product(0, 3, gm, att_ref)
    w_x_stage(0, 2)
    w_product(0, 0, gm, att_ref)
    w_x_stage(0, 3)
    tick(3)
    for load in loads[:-1]:
        load.wait()
    if_outer(mix_step, 1)

    kv_sum[...] = jnp.zeros(kv_sum.shape, jnp.float32)
    table = (table_ref[0], table_ref[1])

    for index in range(2):
        cols = pl.ds(index * (cols_here // 2), cols_here // 2)
        gq[:, cols] = dot_nn(gm[...], o_w[:, cols]).astype(jnp.bfloat16)

    def attend_back(index):
        cols = pl.ds(index * head, head)
        grad_vals = gq[:, cols]
        rotated = rot_ref[:, cols]
        probs = head_probs(rotated, key_ref[...], allow_ref[...])
        grad_probs = matmul_nt(grad_vals, val_ref[...])
        delta = jnp.sum(probs * grad_probs, axis=-1, keepdims=True)
        grad_scores = (probs * (grad_probs - delta)).astype(jnp.bfloat16)
        grad_rot = dot_nn(grad_scores, key_ref[...])
        gq[:, cols] = (spin_back(grad_rot, table) * head_scale).astype(jnp.bfloat16)
        kv_sum[0] += matmul_tn(grad_scores, rotated)
        kv_sum[1] += matmul_tn(probs.astype(jnp.bfloat16), grad_vals)

    between = {
        0: lambda: (w_x_stage(0, 0), tick(4)),
        1: lambda: (tick(5), if_outer(mix_step, 2)),
        2: lambda: if_inner(mix_step, 1),
        4: lambda: (if_outer(mix_step, 3), if_outer(w_z_stage, 0, 1)),
    }
    for index in range(heads):
        attend_back(index)
        if index in between:
            between[index]()
    gkv[:, :head] = spin_back(kv_sum[0], table).astype(jnp.bfloat16)
    gkv[:, head:] = kv_sum[1].astype(jnp.bfloat16)

    w_product(1, 1, n1_ref, gq)
    w_product(1, 2, n1_ref, gq)
    w_x_stage(1, 1)
    w_product(1, 3, n1_ref, gq)
    w_x_stage(1, 2)
    if_outer(w_z_stage, 0, 2)
    w_product(1, 0, n1_ref, gq)
    w_x_stage(1, 3)
    w_x_stage(1, 0)
    for kind in range(3):
        f_x_own(kind).start()

    gm_y.wait_send()
    back = gm
    def input_tile(index, carry):
        at = pl.ds(pl.multiple_of(index * span, 128), span)
        back[:, at] = (
            matmul_nt(gq[...], q_w[at, :]) + matmul_nt(gkv[...], kv_w[index].reshape(span, 2 * head))
        ).astype(jnp.bfloat16)
        return carry

    lax.fori_loop(0, z_size, input_tile, 0)
    back_out = remote(back.at[theirs], back_y, y_send.at[1], y_recv.at[1], to_y)
    back_out.start()

    kv_part = kv_w

    def kv_tile(index, carry):
        at = pl.ds(pl.multiple_of(index * span, 128), span)
        product = dot_nn(n1_ref[:, at].T, gkv[...]).astype(jnp.bfloat16)
        kv_part[index] = product.reshape(kv_part.shape[1:])
        return carry

    lax.fori_loop(0, z_size, kv_tile, 0)
    kv_over_y = remote(kv_part.at[:, :, :, 1 - me_y], kv_y, y_send.at[2], y_recv.at[2], to_y)
    kv_over_y.start()
    if_outer(w_z_stage, 0, 3)
    if_inner(mix_step, 2)

    back_out.wait_recv()

    def input_rows(index, total):
        at = pl.ds(pl.multiple_of(index * 32, 32), 32)
        there = pl.ds(pl.multiple_of(me_y * own + index * 32, 32), 32)
        upstream = back[there, :].astype(jnp.float32) + back_y[at, :].astype(jnp.float32)
        grad, gain_part = norm_back(
            tok_ref[at, :].astype(jnp.float32), gain_ref[0:1, :], upstream
        )
        tgrad_ref[at, :] = (gm_f[at, :] + grad).astype(jnp.bfloat16)
        return total + gain_part

    attn_gain_part = lax.fori_loop(
        0, own // 32, input_rows, jnp.zeros((1, width), jnp.float32)
    )
    for index in range(4):
        at = slice(index * span, (index + 1) * span)
        gain_own[0, index : index + 1, :] = attn_gain_part[:, at]
        gain_own[0, 4 + index : 5 + index, :] = gain_part_ref[4 + index : 5 + index, :]

    def gain_send(stage, where):
        return remote(
            gain_own.at[stage], gain_in.at[stage], g_send.at[stage], g_recv.at[stage], where
        )

    gain_hops = [gain_send(0, to_y), gain_send(1, to_c), gain_send(2, to_x)]
    gain_last = [
        remote(
            gain_own.at[3], gain_in.at[2 + step], g_send.at[2 + step], g_recv.at[2 + step], to_z(step)
        )
        for step in range(1, z_size)
    ]

    def gain_fold(stage):
        gain_hops[stage].wait_recv()
        gain_own[stage + 1] = gain_own[stage] + gain_in[stage]

    gain_hops[0].start()
    mid_load.start()
    if_outer(w_z_stage, 1, 1)
    if_inner(mix_step, 3)
    if_outer(w_z_stage, 1, 2)
    gain_fold(0)
    gain_hops[1].start()
    if_outer(w_z_stage, 1, 3)
    if_inner(w_z_stage, 0, 1)
    gain_fold(1)
    gain_hops[2].start()
    kv_over_y.wait_recv()

    def kv_add_y(index, carry):
        for x_at in range(2):
            for c_at in range(2):
                block = kv_part.at[index, x_at, c_at, me_y]
                block[...] = (
                    block[...].astype(jnp.float32) + kv_y[index, x_at, c_at].astype(jnp.float32)
                ).astype(jnp.bfloat16)
        return carry

    lax.fori_loop(0, z_size, kv_add_y, 0)
    kv_over_c = remote(
        kv_part.at[:, :, 1 - me_c, me_y], kv_c, kc_send.at[0], kc_recv.at[0], to_c
    )
    kv_over_c.start()
    if_inner(w_z_stage, 0, 2)
    gain_fold(2)
    for copy in gain_last:
        copy.start()
    kv_over_c.wait_recv()

    def kv_add_c(index, carry):
        for x_at in range(2):
            block = kv_part.at[index, x_at, me_c, me_y]
            block[...] = (
                block[...].astype(jnp.float32) + kv_c[index, x_at].astype(jnp.float32)
            ).astype(jnp.bfloat16)
        return carry

    lax.fori_loop(0, z_size, kv_add_c, 0)
    kv_over_x = remote(
        kv_part.at[:, 1 - me_x, me_c, me_y], kv_x, kc_send.at[1], kc_recv.at[1], to_x
    )
    kv_over_x.start()
    if_inner(w_z_stage, 0, 3)
    if_inner(w_z_stage, 1, 1)
    mix_step(0)
    kv_over_x.wait_recv()

    def kv_add_x(index, carry):
        block = kv_part.at[index, me_x, me_c, me_y]
        block[...] = (
            block[...].astype(jnp.float32) + kv_x[index].astype(jnp.float32)
        ).astype(jnp.bfloat16)
        return carry

    lax.fori_loop(0, z_size, kv_add_x, 0)
    kv_over_z = [
        remote(
            kv_part.at[lax.rem(me_z + step, z_size), me_x, me_c, me_y],
            kv_z.at[step - 1],
            kz_send.at[step],
            kz_recv.at[step],
            to_z(step),
        )
        for step in range(1, z_size)
    ]
    for copy in kv_over_z:
        copy.start()
    if_inner(w_z_stage, 1, 2)
    w_z_stage(0, 0)
    if_inner(w_z_stage, 1, 3)
    w_z_stage(1, 0)
    for copy in gain_last:
        copy.wait_recv()
    gsum_ref[...] = gain_own[3] + gain_in[3] + gain_in[4] + gain_in[5]
    for copy in kv_over_z:
        copy.wait_recv()
    kvg_ref[...] = (
        kv_part[me_z, me_x, me_c, me_y].astype(jnp.float32)
        + kv_z[0].astype(jnp.float32)
        + kv_z[1].astype(jnp.float32)
        + kv_z[2].astype(jnp.float32)
    )

    back_out.wait_send()
    kv_over_y.wait_send()
    kv_over_c.wait_send()
    kv_over_x.wait_send()
    for kind in range(3):
        f_x_own(kind).wait()
    for index in range(len(tasks)):
        f_x(index).wait_send()
    for step in range(1, z_size):
        for kind in range(3):
            f_z(step, kind, me_z, lambda copy: copy.wait_send())
            f_z(step, kind, behind(step), lambda copy: copy.wait_recv())
    for copy in gain_hops + gain_last + kv_over_z:
        copy.wait_send()
    for step in range(z_size):
        mix_over_y(step).wait_send()
        if step:
            mix_over_z(step).wait_send()
        for kind in range(2):
            w_c(kind, step, 0).wait_send()
            w_c(kind, step, 1).wait_send()
            w_x(kind, step).wait_send()
            if step:
                w_z(kind, step).wait_send()


def post_call(
    tokens,
    gains,
    gain_part,
    normed_one,
    rotated,
    keys,
    values,
    attn_vals,
    table,
    allowed,
    kv_weight,
    query_weight,
    out_weight,
    mix_parts,
    grad_mid,
    grad_mid_low,
    mid,
    ffn_sums,
    main,
):
    z_size = lax.axis_size("z")
    own, width = tokens.shape
    seq = 2 * own
    head = keys.shape[1]
    cols = attn_vals.shape[1]
    rows = width // (4 * z_size)
    units = ffn_sums.shape[4]
    low = lambda *dims: pltpu.VMEM(dims, jnp.bfloat16)
    full = lambda *dims: pltpu.VMEM(dims, jnp.float32)
    out_full = lambda *dims: jax.ShapeDtypeStruct(dims, jnp.float32)
    out_low = lambda *dims: jax.ShapeDtypeStruct(dims, jnp.bfloat16)
    dma = lambda *lead: pltpu.SemaphoreType.DMA(lead)
    vmem = pl.BlockSpec(memory_space=pltpu.VMEM)
    hbm = pl.BlockSpec(memory_space=pl.ANY)
    z = z_size
    return pl.pallas_call(
        functools.partial(post_kernel, z_size, main),
        out_shape=(
            out_low(own, width),
            out_low(own, width),
            out_full(8, width // z),
            out_full(rows // 2, 2 * head),
            out_full(rows, cols),
            out_full(rows, cols),
            out_low(3, z, rows, units),
        ),
        in_specs=[vmem] * 10 + [hbm] * 8,
        out_specs=(vmem,) * 6 + (hbm,),
        scratch_shapes=[
            low(z, 2, 2, 2, rows // 2, 2 * head),
            low(width, cols),
            low(width, cols),
            low(width, cols),
            low(seq, width),
            full(own, width),
            low(seq, cols),
            low(seq, 2 * head),
            full(2, seq, head),
            low(own, width),
            low(z, width, own),
            low(z + 1, width, own),
            low(z, width, own),
            low(z, 2, rows, cols),
            low(z, rows, cols),
            low(z + 1, rows, cols),
            low(z, 2, rows, cols),
            low(z, rows, cols),
            low(z + 1, rows, cols),
            low(z, 2, 2, rows // 2, 2 * head),
            low(z, 2, rows // 2, 2 * head),
            low(z, rows // 2, 2 * head),
            low(z - 1, rows // 2, 2 * head),
            full(4, 8, width // z),
            full(6, 8, width // z),
            low(6, rows, units),
            low(2, rows, units),
            dma(6 + z),
            dma(2),
            dma(9),
            dma(9),
            dma(3, z),
            dma(3, z),
            dma(3),
            dma(3),
            dma(z),
            dma(z),
            dma(z),
            dma(z + 1),
            dma(2, z, 2),
            dma(2, z, 2),
            dma(2, z),
            dma(2, z),
            dma(2, z),
            dma(2, z + 1),
            dma(2),
            dma(2),
            dma(z),
            dma(z),
            dma(6),
            dma(6),
        ],
        compiler_params=pltpu.CompilerParams(
            collective_id=2, has_side_effects=True, vmem_limit_bytes=VMEM_BYTES
        ),
        cost_estimate=pl.CostEstimate(
            flops=14 * seq * width * cols,
            bytes_accessed=10 * width * cols,
            transcendentals=seq * seq * cols // head,
        ),
    )(
        tokens,
        gains,
        gain_part,
        normed_one,
        rotated,
        keys,
        values,
        attn_vals,
        table,
        allowed,
        kv_weight.reshape(z, 2, 2, 2, rows // 2, kv_weight.shape[1]),
        query_weight,
        out_weight,
        mix_parts,
        grad_mid,
        grad_mid_low,
        mid,
        ffn_sums,
    )


def layout_kernel(
    z_size,
    main,
    sum_ref,
    ffn_ref,
    q_ref,
    o_ref,
    kv_ref,
    mixed_in,
    tgrad_in,
    wg_ref,
    wu_ref,
    wd_ref,
    qg_ref,
    og_ref,
    kvg_ref,
    mixed_ref,
    tgrad_ref,
):
    me_z = lax.axis_index("z")
    for kind, out in enumerate((wg_ref, wu_ref, wd_ref)):
        for step in range(z_size):
            at = lax.rem(me_z - step + z_size, z_size)
            values = ffn_ref[kind, step].astype(jnp.float32)
            if step == 0:
                values = values + sum_ref[kind, 0, 0].astype(jnp.float32)
            body = pl.ds(pl.multiple_of(at * main, 128), main)
            out[:, body] = values[:, :main]

            @pl.when((at > 0) & (at < z_size - 1))
            def _(out=out, at=at, values=values):
                tail = z_size * main + lax.rem(at + 1, 2) * 128
                out[:, pl.ds(pl.multiple_of(tail, 128), 128)] = values[:, main:]
    qg_ref[...] = q_ref[...]
    og_ref[...] = o_ref[...]
    kvg_ref[...] = kv_ref[...]
    mixed_ref[...] = mixed_in[...]
    tgrad_ref[...] = tgrad_in[...]


def layout_call(ffn_sums, ffn_grads, query_grad, out_grad, kv_grad, mixed, tokens_grad, ffn_cols):
    z_size = lax.axis_size("z")
    main, units = ragged_split(ffn_cols, z_size)
    rows, cols = query_grad.shape
    parts = rows // 32
    kv_rows = kv_grad.shape[0] // parts
    full = lambda *dims: jax.ShapeDtypeStruct(dims, jnp.float32)
    row = lambda height, width: pl.BlockSpec((height, width), lambda index: (index, 0))
    own, width = mixed.shape
    share = pl.BlockSpec((own, width // parts), lambda index: (0, index))
    specs = [row(32, cols), row(32, cols), row(kv_rows, kv_grad.shape[1]), share, share]
    return pl.pallas_call(
        functools.partial(layout_kernel, z_size, main),
        grid=(parts,),
        out_shape=(
            *[full(rows, ffn_cols)] * 3,
            full(rows, cols),
            full(rows, cols),
            full(*kv_grad.shape),
            jax.ShapeDtypeStruct(mixed.shape, jnp.bfloat16),
            jax.ShapeDtypeStruct(mixed.shape, jnp.bfloat16),
        ),
        in_specs=[
            pl.BlockSpec((3, 1, 1, 32, units), lambda index: (0, 0, 0, index, 0)),
            pl.BlockSpec((3, z_size, 32, units), lambda index: (0, 0, index, 0)),
            *specs,
        ],
        out_specs=(*[row(32, ffn_cols)] * 3, *specs),
        compiler_params=pltpu.CompilerParams(vmem_limit_bytes=VMEM_BYTES),
    )(ffn_sums, ffn_grads, query_grad, out_grad, kv_grad, mixed, tokens_grad)


FF_SPLIT = 4


def ffn_pass(normed, grad_out, gate_weight, up_weight, down_weight):
    gate = jnp.dot(normed, gate_weight, preferred_element_type=jnp.float32)
    up_proj = jnp.dot(normed, up_weight, preferred_element_type=jnp.float32)
    grad_hidden = jnp.dot(grad_out, down_weight, preferred_element_type=jnp.float32)
    product, pull = jax.vjp(gelu_product, gate, up_proj)
    hidden = product.astype(jnp.bfloat16)
    grad_gate_f, grad_up_f = pull(grad_hidden)
    grad_gate = grad_gate_f.astype(jnp.bfloat16)
    grad_up = grad_up_f.astype(jnp.bfloat16)
    mixed_part = matmul_nt(hidden, down_weight).astype(jnp.bfloat16)
    normed_part = (matmul_nt(grad_gate, gate_weight) + matmul_nt(grad_up, up_weight)).astype(
        jnp.bfloat16
    )
    weight_parts = [
        matmul_tn(normed, grad_gate).astype(jnp.bfloat16),
        matmul_tn(normed, grad_up).astype(jnp.bfloat16),
        matmul_tn(grad_out, hidden).astype(jnp.bfloat16),
    ]
    return mixed_part, normed_part, weight_parts


def shards_general(
    tokens,
    segments,
    positions,
    cotangent,
    attn_gain,
    ffn_gain,
    w_kv,
    w_query,
    w_out,
    w_gate,
    w_up,
    w_down,
):
    everywhere = ("z", "xc", "mp")
    dp = ("z", "xc")
    z_size = lax.axis_size("z")
    xc_size = lax.axis_size("xc")
    gains = lax.all_gather(
        jnp.stack([attn_gain, ffn_gain], axis=1), everywhere, axis=0, tiled=True
    ).astype(jnp.float32)
    gain_one, gain_two = gains[:, 0], gains[:, 1]
    kv_weight = lax.all_gather(w_kv, everywhere, axis=0, tiled=True)
    head_dim = kv_weight.shape[1] // 2
    width = tokens.shape[1]
    seq_len = segments.shape[0]
    heads_here = w_query.shape[1] // head_dim
    scale = head_dim ** (-0.5)
    cosine, sine = rotary_angles(positions, head_dim)
    inputs_f = tokens.astype(jnp.float32)
    tokens_all = lax.all_gather(tokens, "mp", axis=0, tiled=True)
    normed_one = norm_gain(tokens_all.astype(jnp.float32), gain_one).astype(jnp.bfloat16)
    query_weight = lax.all_gather(w_query, dp, axis=0, tiled=True)
    out_weight = lax.all_gather(w_out, dp, axis=0, tiled=True)

    rows = w_gate.shape[0]
    unit = w_gate.shape[1] // z_size

    def spread(weight):
        pieces = weight.reshape(rows, z_size, unit).transpose(1, 0, 2)
        pieces = lax.all_to_all(pieces, "z", split_axis=0, concat_axis=0, tiled=True)
        return lax.all_gather(pieces, "xc", axis=1, tiled=False).reshape(width, unit)

    gate_weight, up_weight, down_weight = spread(w_gate), spread(w_up), spread(w_down)
    grad_all = lax.all_gather(cotangent, ("z", "mp"), axis=0, tiled=True)

    query = jnp.dot(normed_one, query_weight, preferred_element_type=jnp.float32).reshape(
        seq_len, heads_here, head_dim
    )
    rotated = (rotate(query, cosine[:, None], sine[:, None]) * scale).astype(jnp.bfloat16)
    keyval = jnp.dot(normed_one, kv_weight, preferred_element_type=jnp.float32)
    keys = rotate(keyval[:, :head_dim], cosine, sine).astype(jnp.bfloat16)
    values = keyval[:, head_dim:].astype(jnp.bfloat16)
    allowed = block_allowed(segments, 0, seq_len)
    scores = jnp.einsum("thd,sd->hts", rotated, keys, preferred_element_type=jnp.float32)
    scores = jnp.where(allowed[None], scores, masked_score)
    row_max = jnp.max(scores, axis=-1, keepdims=True)
    weights = jnp.exp(scores - row_max)
    probs = weights / jnp.sum(weights, axis=-1, keepdims=True)
    probs_low = probs.astype(jnp.bfloat16)
    attn_vals = (
        jnp.einsum("hts,sd->thd", probs_low, values, preferred_element_type=jnp.float32)
        .reshape(seq_len, heads_here * head_dim)
        .astype(jnp.bfloat16)
    )
    mid = inputs_f + lax.psum_scatter(
        matmul_nt(attn_vals, out_weight).astype(jnp.bfloat16),
        "mp",
        scatter_dimension=0,
        tiled=True,
    ).astype(jnp.float32)
    normed_two = norm_gain(mid, gain_two).astype(jnp.bfloat16)
    normed_all = lax.all_gather(normed_two, ("z", "mp"), axis=0, tiled=True)

    mixed_part, normed_part, weight_parts = ffn_pass(
        normed_all, grad_all, gate_weight, up_weight, down_weight
    )
    grad_normed_two = lax.psum_scatter(
        normed_part, ("z", "mp"), scatter_dimension=0, tiled=True
    ).astype(jnp.float32)
    mixed = (
        mid
        + lax.psum_scatter(mixed_part, ("z", "mp"), scatter_dimension=0, tiled=True).astype(
            jnp.float32
        )
    ).astype(jnp.bfloat16)

    def collect(part):
        pieces = part.reshape(z_size, xc_size, rows, unit).transpose(1, 0, 2, 3)
        pieces = pieces.reshape(xc_size * z_size * rows, unit)
        pieces = lax.psum_scatter(pieces, "xc", scatter_dimension=0, tiled=True)
        pieces = pieces.reshape(z_size, rows, unit)
        pieces = lax.all_to_all(pieces, "z", split_axis=0, concat_axis=0, tiled=True)
        return pieces.transpose(1, 0, 2).reshape(rows, z_size * unit).astype(jnp.float32)

    w_gate_grad, w_up_grad, w_down_grad = [collect(part) for part in weight_parts]

    norm_pull_two = jax.vjp(norm_gain, mid, gain_two)[1]
    grad_mid_norm, grad_gain_two = norm_pull_two(grad_normed_two)
    grad_mid = cotangent.astype(jnp.float32) + grad_mid_norm
    grad_mid_all = lax.all_gather(grad_mid.astype(jnp.bfloat16), "mp", axis=0, tiled=True)
    grad_vals = (
        jnp.dot(grad_mid_all, out_weight, preferred_element_type=jnp.float32)
        .astype(jnp.bfloat16)
        .reshape(seq_len, heads_here, head_dim)
    )
    grad_probs = jnp.einsum("thd,sd->hts", grad_vals, values, preferred_element_type=jnp.float32)
    delta = jnp.sum(probs * grad_probs, axis=-1, keepdims=True)
    grad_scores = (probs * (grad_probs - delta)).astype(jnp.bfloat16)
    grad_rot = jnp.einsum("hts,sd->thd", grad_scores, keys, preferred_element_type=jnp.float32)
    key_sum = jnp.einsum("hts,thd->sd", grad_scores, rotated, preferred_element_type=jnp.float32)
    value_sum = jnp.einsum("hts,thd->sd", probs_low, grad_vals, preferred_element_type=jnp.float32)
    grad_query = (
        (unrotate(grad_rot, cosine[:, None], sine[:, None]) * scale)
        .reshape(seq_len, heads_here * head_dim)
        .astype(jnp.bfloat16)
    )
    grad_kv = jnp.concatenate([unrotate(key_sum, cosine, sine), value_sum], axis=1).astype(
        jnp.bfloat16
    )
    grad_normed_one = lax.psum_scatter(
        (matmul_nt(grad_query, query_weight) + matmul_nt(grad_kv, kv_weight)).astype(jnp.bfloat16),
        "mp",
        scatter_dimension=0,
        tiled=True,
    ).astype(jnp.float32)
    norm_pull_one = jax.vjp(norm_gain, inputs_f, gain_one)[1]
    grad_input_norm, grad_gain_one = norm_pull_one(grad_normed_one)
    tokens_grad = (grad_mid + grad_input_norm).astype(jnp.bfloat16)

    w_query_grad = lax.psum_scatter(
        matmul_tn(normed_one, grad_query).astype(jnp.bfloat16), dp, scatter_dimension=0, tiled=True
    ).astype(jnp.float32)
    w_out_grad = lax.psum_scatter(
        matmul_tn(grad_mid_all, attn_vals).astype(jnp.bfloat16), dp, scatter_dimension=0, tiled=True
    ).astype(jnp.float32)
    small = jnp.concatenate(
        [matmul_tn(normed_one, grad_kv), grad_gain_one[:, None], grad_gain_two[:, None]], axis=1
    )
    small = lax.psum_scatter(small, everywhere, scatter_dimension=0, tiled=True)
    kv_grad = small[:, : 2 * head_dim]
    return (
        mixed,
        tokens_grad,
        small[:, 2 * head_dim],
        small[:, 2 * head_dim + 1],
        kv_grad,
        w_query_grad,
        w_out_grad,
        w_gate_grad,
        w_up_grad,
        w_down_grad,
    )


def shards_fast(
    tokens,
    segments,
    positions,
    cotangent,
    attn_gain,
    ffn_gain,
    w_kv,
    w_query,
    w_out,
    w_gate,
    w_up,
    w_down,
):
    seq_len = segments.shape[0]
    cosine, sine = rotary_angles(positions, w_kv.shape[1] // 2)
    table = jnp.stack(
        [
            jnp.concatenate([cosine, cosine], axis=1),
            jnp.concatenate([-sine, sine], axis=1),
        ]
    )
    gain_rows = jnp.pad(
        jnp.stack([attn_gain, ffn_gain]).astype(jnp.float32),
        ((0, 6), (0, 128 - attn_gain.shape[0])),
    )
    segment_rows = jnp.broadcast_to(segments.astype(jnp.float32)[None, :], (8, seq_len))
    (
        normed_one,
        rotated,
        keys,
        values,
        attn_vals,
        mid,
        normed_two,
        gains,
        allowed,
        kv_weight,
        query_weight,
        out_weight,
        ffn_weights,
        grad_all,
    ) = pre_call(
        tokens,
        w_kv,
        gain_rows,
        table,
        segment_rows,
        cotangent,
        w_query,
        w_out,
        (w_gate, w_up, w_down),
    )
    main = ragged_split(w_gate.shape[1], lax.axis_size("z"))[0]
    grad_mid, gain_part, mix_parts, ffn_sums, grad_mid_low = ffn_call(
        gains, normed_two, grad_all, ffn_weights, mid, w_gate.shape[0], main
    )
    mixed, tokens_grad, gain_grads, kv_grad, query_grad, out_grad, ffn_grads = post_call(
        tokens,
        gains,
        gain_part,
        normed_one,
        rotated,
        keys,
        values,
        attn_vals,
        table,
        allowed,
        kv_weight,
        query_weight,
        out_weight,
        mix_parts,
        grad_mid,
        grad_mid_low,
        mid,
        ffn_sums,
        main,
    )
    *ffn_out, query_grad, out_grad, kv_grad, mixed, tokens_grad = layout_call(
        ffn_sums,
        ffn_grads,
        query_grad,
        out_grad,
        kv_grad,
        mixed,
        tokens_grad,
        w_gate.shape[1],
    )
    share = attn_gain.shape[0]
    place = lax.axis_index(("z", "x", "c", "mp")) * share
    gain_grads = gain_grads.reshape(2, gain_grads.size // 2)
    gain_grads = lax.dynamic_slice(gain_grads, (0, place), (2, share))
    return (
        mixed,
        tokens_grad,
        gain_grads[0],
        gain_grads[1],
        kv_grad,
        query_grad,
        out_grad,
        *ffn_out,
    )


def solution(mesh):
    dp_size, mp_size = mesh.shape["dp"], mesh.shape["mp"]
    if dp_size == 4 * FF_SPLIT and mp_size == 2:
        body, dp = shards_fast, ("z", "x", "c")
        sizes = (FF_SPLIT, 2, 2, mp_size)
    else:
        body, dp = shards_general, ("z", "xc")
        sizes = (FF_SPLIT, dp_size // FF_SPLIT, mp_size)
    all_axes = (*dp, "mp")
    fine = jax.sharding.Mesh(mesh.devices.reshape(sizes), all_axes)
    in_specs = (
        P(all_axes, None),
        P(dp),
        P(dp),
        P(all_axes, None),
        P(all_axes),
        P(all_axes),
        P(all_axes, None),
        P(dp, "mp"),
        P(dp, "mp"),
        P(dp, "mp"),
        P(dp, "mp"),
        P(dp, "mp"),
    )
    out_specs = (
        P(all_axes, None),
        P(all_axes, None),
        P(all_axes),
        P(all_axes),
        P(all_axes, None),
        P(dp, "mp"),
        P(dp, "mp"),
        P(dp, "mp"),
        P(dp, "mp"),
        P(dp, "mp"),
    )
    return jax.shard_map(body, mesh=fine, in_specs=in_specs, out_specs=out_specs, check_vma=False)
```

```python
import functools

import jax
import jax.numpy as jnp
from jax import lax
from jax.experimental import pallas as pl
from jax.experimental.pallas import tpu as pltpu
from jax.sharding import PartitionSpec as P

WINDOW = 2048


epsilon = 1e-06
rope_base = 10000.0
masked_score = -1e30
VMEM_BYTES = 66_000_000


def norm_gain(values, gain):
    return values * lax.rsqrt(jnp.mean(values * values, axis=-1, keepdims=True) + epsilon) * gain


def rotary_angles(positions, head_width):
    quarter = head_width // 4
    freqs = rope_base ** (-jnp.arange(quarter).astype(jnp.float32) / quarter)
    phase = positions.astype(jnp.float32)[:, None] * freqs[None, :]
    return (jnp.cos(phase), jnp.sin(phase))


def rotate(values, cosine, sine):
    quarter = cosine.shape[-1]
    first_half = values[..., :quarter]
    second_half = values[..., quarter : 2 * quarter]
    return jnp.concatenate(
        [
            first_half * cosine - second_half * sine,
            second_half * cosine + first_half * sine,
            values[..., 2 * quarter :],
        ],
        axis=-1,
    )


def unrotate(values, cosine, sine):
    quarter = cosine.shape[-1]
    first_half = values[..., :quarter]
    second_half = values[..., quarter : 2 * quarter]
    return jnp.concatenate(
        [
            first_half * cosine + second_half * sine,
            second_half * cosine - first_half * sine,
            values[..., 2 * quarter :],
        ],
        axis=-1,
    )


def gelu_product(gate, up_proj):
    return jax.nn.gelu(gate, approximate=True) * up_proj


def matmul_nt(left, right):
    return lax.dot_general(
        left, right, (((1,), (1,)), ((), ())), preferred_element_type=jnp.float32
    )


def matmul_tn(left, right):
    return lax.dot_general(
        left, right, (((0,), (0,)), ((), ())), preferred_element_type=jnp.float32
    )


def block_allowed(segments, first_row, rows):
    seq_len = segments.shape[0]
    query_rows = first_row + jnp.arange(rows)
    key_rows = jnp.arange(seq_len)
    return (
        (segments[:, None] == segments[None, :])
        & (key_rows[None, :] <= query_rows[:, None])
        & (query_rows[:, None] - key_rows[None, :] < WINDOW)
    )


MESH_ID = pl.DeviceIdType.MESH
GELU_A = 0.7978845608028654
GELU_B = 0.044715
TILE = 256
WIDE = 512


def remote(src, dst, send_sem, recv_sem, where):
    return pltpu.make_async_remote_copy(
        src_ref=src,
        dst_ref=dst,
        send_sem=send_sem,
        recv_sem=recv_sem,
        device_id=where,
        device_id_type=MESH_ID,
    )


def dot_nn(left, right):
    return lax.dot_general(
        left, right, (((1,), (0,)), ((), ())), preferred_element_type=jnp.float32
    )


def gelu_parts(gate):
    square = gate * gate
    bend = jnp.tanh(GELU_A * gate * (1.0 + GELU_B * square))
    half = 0.5 * (1.0 + bend)
    slope = half + 0.5 * gate * (1.0 - bend * bend) * GELU_A * (1.0 + 3.0 * GELU_B * square)
    return gate * half, slope


def add_rows(first, rest, out, count):
    def body(index, carry):
        step = pl.ds(pl.multiple_of(index * 32, 32), 32)
        total = first[step, :].astype(jnp.float32)
        for other in rest:
            total = total + other[step, :].astype(jnp.float32)
        out[step, :] = total.astype(out.dtype)
        return carry

    lax.fori_loop(0, count // 32, body, 0)


def norm_back(values, gain, upstream):
    scale = lax.rsqrt(jnp.mean(values * values, axis=-1, keepdims=True) + epsilon)
    normed = values * scale
    pulled = gain * upstream
    back = scale * (pulled - normed * jnp.mean(normed * pulled, axis=-1, keepdims=True))
    return back, jnp.sum(upstream * normed, axis=0, keepdims=True)


def ffn_kernel(
    z_size,
    main,
    gain_ref,
    own_hbm,
    dy_hbm,
    w_hbm,
    mid_hbm,
    gm_ref,
    gain_part,
    mix_hbm,
    sums_hbm,
    gm_hbm,
    n2,
    dy,
    w3,
    h3,
    n2_t,
    dy_t,
    gn_part,
    mix_buf,
    gn_y,
    gn_z,
    gn_s,
    c_in,
    x_in,
    mid,
    load_sem,
    mix_sem,
    ag_y_send,
    ag_y_recv,
    ag_z_send,
    ag_z_recv,
    rs_y_send,
    rs_y_recv,
    rs_z_send,
    rs_z_recv,
    c_send,
    c_recv,
    x_send,
    x_recv,
    out_sem,
):
    own = own_hbm.shape[0] // 2
    width = own_hbm.shape[1]
    units = w3.shape[2]
    rows = c_in.shape[3]
    span = width // z_size
    me_y, me_z = lax.axis_index("mp"), lax.axis_index("z")
    me_x, me_c = lax.axis_index("x"), lax.axis_index("c")
    mine = pl.ds(pl.multiple_of(me_y * own, own), own)
    theirs = pl.ds(pl.multiple_of((1 - me_y) * own, own), own)
    to_y, to_x, to_c = {"mp": 1 - me_y}, {"x": 1 - me_x}, {"c": 1 - me_c}

    def ahead(step):
        return lax.rem(me_z + step, z_size)

    def to_z(step):
        return {"z": ahead(step)}

    def row_block(z_at, x_at, c_at):
        return pl.ds(pl.multiple_of(((z_at * 2 + x_at) * 2 + c_at) * rows, rows), rows)

    inner = (me_z > 0) & (me_z < z_size - 1)
    outer = (me_z == 0) | (me_z == z_size - 1)

    def w_load(index, columns):
        cols = pl.ds(0, columns)
        return pltpu.make_async_copy(
            w_hbm.at[index, :, cols], w3.at[index, :, cols], load_sem.at[z_size + index]
        )

    def w_loads(act):
        for case, columns in ((inner, units), (outer, main)):

            @pl.when(case)
            def _(columns=columns):
                for index in range(3):
                    act(w_load(index, columns))

    w_loads(lambda copy: copy.start())
    dy_loads = [
        pltpu.make_async_copy(dy_hbm.at[index], dy, load_sem.at[index])
        for index in range(z_size)
    ]
    own_load = pltpu.make_async_copy(own_hbm, n2.at[0], load_sem.at[z_size + 3])
    mid_load = pltpu.make_async_copy(mid_hbm, mid, load_sem.at[z_size + 4])
    for load in (own_load, dy_loads[0], mid_load):
        load.start()

    barrier = pltpu.get_barrier_semaphore()
    peers = [to_y, to_x, to_c] + [to_z(step) for step in range(1, z_size)]
    for where in peers:
        pl.semaphore_signal(barrier, inc=1, device_id=where, device_id_type=MESH_ID)
    pl.semaphore_wait(barrier, len(peers))

    def ag_y(index):
        block = n2.at[index, mine]
        return remote(block, block, ag_y_send.at[index], ag_y_recv.at[index], to_y)

    def ag_y_in(index):
        block = n2.at[index, theirs]
        return remote(block, block, ag_y_send.at[index], ag_y_recv.at[index], to_y)

    def ag_z(index):
        src = own_hbm.at[mine] if index == 0 else n2.at[index, mine]
        return remote(
            src, n2.at[index + 1, mine], ag_z_send.at[index], ag_z_recv.at[index + 1], to_z(1)
        )

    def ag_z_in(index):
        block = n2.at[index, mine]
        return remote(block, block, ag_z_send.at[0], ag_z_recv.at[index], to_z(1))

    def ag_last():
        return remote(
            n2.at[2, theirs], n2.at[3, theirs], ag_y_send.at[3], ag_y_recv.at[3], to_z(1)
        )

    def forward(index):
        ag_z_in(index).wait_recv()
        ag_z(index).start()
        ag_y(index).start()

    ag_z(0).start()

    mix_copies = []

    def chunk(index):
        if index:
            mix_copies[index - 1].wait()
        dy_loads[index].wait()
        rows_at = pl.ds(index * 2 * own, 2 * own)

        def up_tile(tile, carry):
            cols = pl.ds(pl.multiple_of(tile * TILE, TILE), TILE)
            gate = dot_nn(n2[index], w3[0, :, cols])
            up_proj = dot_nn(n2[index], w3[1, :, cols])
            grad_hidden = dot_nn(dy[...], w3[2, :, cols])
            act, slope = gelu_parts(gate)
            h3[0, rows_at, cols] = (grad_hidden * up_proj * slope).astype(jnp.bfloat16)
            h3[1, rows_at, cols] = (grad_hidden * act).astype(jnp.bfloat16)
            h3[2, rows_at, cols] = (act * up_proj).astype(jnp.bfloat16)
            part = pl.ds(pl.multiple_of(tile * span, 128), span)
            n2_t[part, rows_at] = n2[index, :, part].T
            dy_t[part, rows_at] = dy[:, part].T
            return carry

        lax.fori_loop(0, units // TILE, up_tile, 0)

        def down_tile(tile, carry):
            at = pl.ds(pl.multiple_of(tile * span, 128), span)
            normed = matmul_nt(w3[0, at, :], h3[0, rows_at, :]) + matmul_nt(
                w3[1, at, :], h3[1, rows_at, :]
            )
            mixed = matmul_nt(w3[2, at, :], h3[2, rows_at, :])
            for half in range(2):
                cols = slice(half * own, (half + 1) * own)
                gn_part[index, half, at, :] = normed[:, cols].astype(jnp.bfloat16)
                mix_buf[half, at, :] = mixed[:, cols].astype(jnp.bfloat16)
            return carry

        for half in range(2):
            lax.fori_loop(half * z_size // 2, (half + 1) * z_size // 2, down_tile, 0)
            if index:
                rs_y(index, half).start()
        copy = pltpu.make_async_copy(mix_buf, mix_hbm.at[index], mix_sem.at[index])
        copy.start()
        mix_copies.append(copy)
        if index + 1 < z_size:
            dy_loads[index + 1].start()

    def half_of(half):
        return pl.ds(half * width // 2, width // 2)

    def rs_y(index, half):
        at = half_of(half)
        return remote(
            gn_part.at[index, 1 - me_y, at],
            gn_y.at[index, at],
            rs_y_send.at[index, half],
            rs_y_recv.at[index, half],
            to_y,
        )

    def rs_z(index, half):
        at = half_of(half)
        return remote(
            gn_s.at[index - 1, at],
            gn_z.at[index - 1, at],
            rs_z_send.at[index, half],
            rs_z_recv.at[index - 1, half],
            to_z(1),
        )

    def rs_z_in(slot, half):
        block = gn_z.at[slot, half_of(half)]
        return remote(block, block, rs_z_send.at[1, half], rs_z_recv.at[slot, half], to_z(1))

    def rs_step(index, half):
        rs_y(index, half).wait_recv()
        slot = (index - 2) % z_size
        if index != 1:
            rs_z_in(slot, half).wait_recv()

        def add_tile(tile, carry):
            at = pl.ds(pl.multiple_of(half * width // 2 + tile * TILE, TILE), TILE)
            total = gn_part[index, me_y, at, :].astype(jnp.float32) + gn_y[index, at, :].astype(
                jnp.float32
            )
            if index != 1:
                total = total + gn_z[slot, at, :].astype(jnp.float32)
            if index == 0:
                gm_ref[:, at] = total.T
            else:
                gn_s[index - 1, at, :] = total.astype(jnp.bfloat16)
            return carry

        lax.fori_loop(0, width // 2 // TILE, add_tile, 0)
        if index != 0:
            rs_z(index, half).start()


    def grads(step):
        at = pl.ds(pl.multiple_of(ahead(step) * span, 128), span)
        for kind, source in enumerate((n2_t, n2_t, dy_t)):

            def tile_body(tile, carry, kind=kind, source=source):
                cols = pl.ds(pl.multiple_of(tile * WIDE, WIDE), WIDE)
                w3[kind, at, cols] = dot_nn(source[at, :], h3[kind, :, cols]).astype(jnp.bfloat16)
                return carry

            lax.fori_loop(0, units // WIDE, tile_body, 0)
        for far in (1, 0):
            for kind in range(3):
                over_c(kind, step, far).start()

    def over_c(kind, step, far):
        x_at = 1 - me_x if far else me_x
        return remote(
            w3.at[kind, row_block(ahead(step), x_at, 1 - me_c)],
            c_in.at[kind, step, far],
            c_send.at[kind, step, far],
            c_recv.at[kind, step, far],
            to_c,
        )

    def over_x(kind):
        return remote(
            w3.at[kind, row_block(ahead(1), 1 - me_x, me_c)],
            x_in.at[kind],
            x_send.at[kind],
            x_recv.at[kind],
            to_x,
        )

    out_copies = []

    def keep(kind, step, far, block):
        copy = pltpu.make_async_copy(
            block, sums_hbm.at[kind, step, far], out_sem.at[kind, step, far]
        )
        copy.start()
        out_copies.append(copy)

    def core_sums(step):
        for far in (1, 0):
            for kind in range(3):
                over_c(kind, step, far).wait_recv()
                x_at = 1 - me_x if far else me_x
                block = w3.at[kind, row_block(ahead(step), x_at, me_c)]
                add_rows(block, [c_in.at[kind, step, far]], block, rows)
                if step != 1:
                    keep(kind, step, far, block)
                elif far:
                    over_x(kind).start()

    def first_sums():
        for kind in range(3):
            over_x(kind).wait_recv()
            block = w3.at[kind, row_block(ahead(1), me_x, me_c)]
            add_rows(block, [x_in.at[kind]], block, rows)
            keep(kind, 1, 0, block)

    own_load.wait()
    w_loads(lambda copy: copy.wait())

    @pl.when(outer)
    def _():
        w3[:, :, main:] = jnp.zeros((3, width, units - main), jnp.bfloat16)

    chunk(0)
    forward(1)
    forward(2)
    ag_y_in(1).wait_recv()
    chunk(1)
    ag_y_in(2).wait_recv()
    ag_last().start()
    chunk(2)
    rs_step(1, 0)
    rs_step(1, 1)
    ag_z_in(3).wait_recv()
    ag_last().wait_recv()
    chunk(3)
    rs_y(0, 0).start()
    rs_y(0, 1).start()
    rs_step(2, 0)
    rs_step(2, 1)
    grads(1)
    rs_step(3, 0)
    grads(2)
    rs_step(3, 1)
    core_sums(1)
    grads(3)
    core_sums(2)
    rs_step(0, 0)
    rs_step(0, 1)

    cot_load = pltpu.make_async_copy(
        dy_hbm.at[0, mine], dy.at[pl.ds(0, own)], load_sem.at[z_size + 3]
    )
    cot_load.start()
    cot_load.wait()
    mid_load.wait()

    def mid_rows(index, total):
        at = pl.ds(pl.multiple_of(index * 32, 32), 32)
        grad, gain_sum = norm_back(mid[at, :], gain_ref[1:2, :], gm_ref[at, :])
        grad = grad + dy[at, :].astype(jnp.float32)
        gm_ref[at, :] = grad
        dy[pl.ds(pl.multiple_of(own + index * 32, 32), 32), :] = grad.astype(jnp.bfloat16)
        return total + gain_sum

    gain_sum = lax.fori_loop(0, own // 32, mid_rows, jnp.zeros((1, width), jnp.float32))
    gm_save = pltpu.make_async_copy(dy.at[pl.ds(own, own)], gm_hbm, load_sem.at[z_size + 3])
    gm_save.start()
    for index in range(4):
        gain_part[index : index + 1, :] = jnp.zeros((1, span), jnp.float32)
        gain_part[4 + index : 5 + index, :] = gain_sum[:, index * span : (index + 1) * span]
    grads(0)
    core_sums(3)
    core_sums(0)
    first_sums()
    gm_save.wait()

    for copy in mix_copies[3:] + out_copies:
        copy.wait()
    for index in range(z_size):
        if index in (1, 2):
            ag_y(index).wait_send()
        if index == 3:
            ag_last().wait_send()
        if index < z_size - 1:
            ag_z(index).wait_send()
        for half in range(2):
            rs_y(index, half).wait_send()
            if index:
                rs_z(index, half).wait_send()
        for kind in range(3):
            over_c(kind, index, 0).wait_send()
            over_c(kind, index, 1).wait_send()
            if index == 1:
                over_x(kind).wait_send()


def ffn_call(gains, normed, grad_all, weights, mid, rows, main):
    z_size = lax.axis_size("z")
    pair, width = normed.shape
    units = weights.shape[2]
    own = pair // 2
    wide = lambda *lead: pltpu.VMEM((*lead, width), jnp.bfloat16)
    tall = lambda *lead: pltpu.VMEM((*lead, width, own), jnp.bfloat16)
    dma = lambda *lead: pltpu.SemaphoreType.DMA(lead)
    vmem = pl.BlockSpec(memory_space=pltpu.VMEM)
    hbm = pl.BlockSpec(memory_space=pl.ANY)
    return pl.pallas_call(
        functools.partial(ffn_kernel, z_size, main),
        out_shape=(
            jax.ShapeDtypeStruct((own, width), jnp.float32),
            jax.ShapeDtypeStruct((8, width // z_size), jnp.float32),
            jax.ShapeDtypeStruct((z_size, 2, width, own), jnp.bfloat16),
            jax.ShapeDtypeStruct((3, z_size, 2, rows, units), jnp.bfloat16),
            jax.ShapeDtypeStruct((own, width), jnp.bfloat16),
        ),
        in_specs=[vmem, hbm, hbm, hbm, hbm],
        out_specs=(vmem, vmem, hbm, hbm, hbm),
        scratch_shapes=[
            wide(z_size, pair),
            wide(pair),
            pltpu.VMEM(weights.shape, jnp.bfloat16),
            pltpu.VMEM((3, z_size * pair, units), jnp.bfloat16),
            pltpu.VMEM((width, z_size * pair), jnp.bfloat16),
            pltpu.VMEM((width, z_size * pair), jnp.bfloat16),
            tall(z_size, 2),
            tall(2),
            tall(z_size),
            tall(z_size - 1),
            tall(z_size - 1),
            pltpu.VMEM((3, z_size, 2, rows, units), jnp.bfloat16),
            pltpu.VMEM((3, rows, units), jnp.bfloat16),
            pltpu.VMEM((own, width), jnp.float32),
            dma(z_size + 5),
            dma(z_size),
            dma(z_size),
            dma(z_size),
            dma(z_size),
            dma(z_size),
            dma(z_size, 2),
            dma(z_size, 2),
            dma(z_size, 2),
            dma(z_size, 2),
            dma(3, z_size, 2),
            dma(3, z_size, 2),
            dma(3),
            dma(3),
            dma(3, z_size, 2),
        ],
        compiler_params=pltpu.CompilerParams(
            collective_id=0, has_side_effects=True, vmem_limit_bytes=VMEM_BYTES
        ),
        cost_estimate=pl.CostEstimate(
            flops=18 * z_size * pair * width * units,
            bytes_accessed=4 * weights.size + 12 * z_size * pair * width,
            transcendentals=z_size * pair * units,
        ),
    )(gains, normed, grad_all, weights, mid)


def spin(values, table):
    first = values[:, : values.shape[1] // 2]
    turned = first * table[0] + pltpu.roll(first, first.shape[1] // 2, 1) * table[1]
    return jnp.concatenate([turned, values[:, values.shape[1] // 2 :]], axis=1)


def spin_back(values, table):
    first = values[:, : values.shape[1] // 2]
    turned = first * table[0] - pltpu.roll(first, first.shape[1] // 2, 1) * table[1]
    return jnp.concatenate([turned, values[:, values.shape[1] // 2 :]], axis=1)


def head_probs(rotated, keys, allowed):
    scores = jnp.where(allowed > 0.5, matmul_nt(rotated, keys), masked_score)
    weights = jnp.exp(scores - jnp.max(scores, axis=-1, keepdims=True))
    return weights / jnp.sum(weights, axis=-1, keepdims=True)


def ragged_split(columns, parts):
    main = columns // parts // 128 * 128
    return main, main + 128


def pre_kernel(
    z_size,
    tok_ref,
    wkv_ref,
    gains_ref,
    table_ref,
    seg_ref,
    cot_hbm,
    wq_hbm,
    wo_hbm,
    wg_hbm,
    wu_hbm,
    wd_hbm,
    n1_ref,
    rot_ref,
    key_ref,
    val_ref,
    att_ref,
    mid_ref,
    n2_ref,
    gain_ref,
    allow_ref,
    kv_out,
    wq_out,
    wo_out,
    w3_out,
    dy_out,
    kv_w,
    q_w,
    o_w,
    tok,
    part,
    part_y,
    query,
    y_send,
    y_recv,
    ky_send,
    ky_recv,
    az_send,
    az_recv,
    ax_send,
    ax_recv,
    ac_send,
    ac_recv,
    fz_send,
    fz_recv,
    fx_send,
    fx_recv,
    fc_send,
    fc_recv,
    dz_send,
    dz_recv,
    dy_send,
    dy_recv,
    local_sem,
):
    me_z, me_x = lax.axis_index("z"), lax.axis_index("x")
    me_c, me_y = lax.axis_index("c"), lax.axis_index("mp")
    own, width = tok_ref.shape
    rows = wq_hbm.shape[0]
    half_rows = wkv_ref.shape[0]
    head = key_ref.shape[1]
    main, units = ragged_split(wg_hbm.shape[1], z_size)
    to_y, to_x, to_c = {"mp": 1 - me_y}, {"x": 1 - me_x}, {"c": 1 - me_c}

    def to_z(step):
        return {"z": lax.rem(me_z + step, z_size)}

    def from_z(step):
        return lax.rem(me_z - step + z_size, z_size)

    def row_block(step, x_at, c_at):
        start = ((from_z(step) * 2 + x_at) * 2 + c_at) * rows
        return pl.ds(pl.multiple_of(start, rows), rows)

    mine = pl.ds(pl.multiple_of(me_y * own, own), own)
    theirs = pl.ds(pl.multiple_of((1 - me_y) * own, own), own)
    bufs = (kv_w, q_w, o_w)
    inputs = (None, wq_hbm, wo_hbm)

    locals_ = []

    def local(src, dst):
        copy = pltpu.make_async_copy(src, dst, local_sem.at[len(locals_)])
        copy.start()
        locals_.append(copy)
        return copy

    here = row_block(0, me_x, me_c)
    own_q = local(wq_hbm, q_w.at[here])
    own_o = local(wo_hbm, o_w.at[here])
    ffn_in = (wg_hbm, wu_hbm, wd_hbm)

    def body_of(target):
        return pl.ds(pl.multiple_of(target * main, 128), main), pl.ds(0, main)

    def tail_of(target):
        start = z_size * main + lax.rem(target + 1, 2) * 128
        return pl.ds(pl.multiple_of(start, 128), 128), pl.ds(main, 128)

    def is_inner(at):
        return (at > 0) & (at < z_size - 1)

    own_f = []
    for kind in range(3):
        src, dst = body_of(me_z)
        own_f.append(local(ffn_in[kind].at[:, src], w3_out.at[kind, here, dst]))

    def own_tail(kind):
        src, dst = tail_of(me_z)
        return pltpu.make_async_copy(
            ffn_in[kind].at[:, src], w3_out.at[kind, here, dst], local_sem.at[12 + kind]
        )

    @pl.when(is_inner(me_z))
    def _():
        for kind in range(3):
            own_tail(kind).start()
    own_d = local(cot_hbm, dy_out.at[0, mine])

    kv_own = pl.ds(pl.multiple_of(here.start + me_y * half_rows, half_rows), half_rows)
    spread = jnp.concatenate([gains_ref[...], jnp.zeros((120, 128), jnp.float32)], axis=0).T
    kv_w[kv_own, : 2 * head] = wkv_ref[...]
    kv_w[kv_own, 2 * head :] = spread[:half_rows, :].astype(jnp.bfloat16)

    barrier = pltpu.get_barrier_semaphore()
    peers = [to_y, to_x, to_c] + [to_z(step) for step in range(1, z_size)]
    for where in peers:
        pl.semaphore_signal(barrier, inc=1, device_id=where, device_id_type=MESH_ID)
    pl.semaphore_wait(barrier, len(peers))

    tok_y = remote(tok_ref, tok.at[mine], y_send.at[1], y_recv.at[1], to_y)
    tok_y_in = remote(tok_ref, tok.at[theirs], y_send.at[1], y_recv.at[1], to_y)
    part_out = remote(part.at[theirs], part_y, y_send.at[2], y_recv.at[2], to_y)
    n2_y = remote(n2_ref.at[mine], n2_ref.at[mine], y_send.at[3], y_recv.at[3], to_y)
    n2_y_in = remote(n2_ref.at[theirs], n2_ref.at[theirs], y_send.at[3], y_recv.at[3], to_y)

    def block_of(kind, step, x_at):
        if kind:
            return row_block(step, x_at, me_c)
        return kv_rows(step, x_at, me_y)

    def kv_rows(step, x_at, y_at):
        start = row_block(step, x_at, me_c).start + y_at * half_rows
        return pl.ds(pl.multiple_of(start, half_rows), half_rows)

    def kv_y(step, far):
        x_at = 1 - me_x if far else me_x
        block = kv_w.at[kv_rows(step, x_at, me_y)]
        slot = step + z_size * far
        return remote(block, block, ky_send.at[slot], ky_recv.at[slot], to_y)

    def kv_y_in(step, far):
        x_at = 1 - me_x if far else me_x
        block = kv_w.at[kv_rows(step, x_at, 1 - me_y)]
        slot = step + z_size * far
        return remote(block, block, ky_send.at[slot], ky_recv.at[slot], to_y)

    def source(kind, step):
        if isinstance(step, int) and step == 0 and kind:
            return inputs[kind]
        return bufs[kind].at[block_of(kind, step, me_x)]

    first_z, last_z = (z_size - 1 - me_z) // (z_size - 1), me_z // (z_size - 1)
    inner = first_z + last_z == 0
    order = (0, 1 + 2 * first_z, 3 - first_z - last_z, 2 - first_z + last_z)
    hops = (
        None,
        (lax.rem(me_z + 1, z_size), 2),
        (lax.rem(me_z + z_size - 1, z_size), 2),
        (lax.rem(3 * (me_z + 3), z_size), lax.rem(2 * me_z + 3, z_size)),
    )

    def a_z_own(kind, right):
        return remote(
            source(kind, 0),
            bufs[kind].at[block_of(kind, 0, me_x)],
            az_send.at[kind, right],
            az_recv.at[kind, 1 if right else z_size - 1],
            to_z(1 if right else z_size - 1),
        )

    def a_z_start(kind):
        @pl.when(last_z == 0)
        def _():
            a_z_own(kind, 1).start()

        @pl.when(first_z == 0)
        def _():
            a_z_own(kind, 0).start()

    def a_z(kind, index):
        target, slot = hops[index]
        block = bufs[kind].at[block_of(kind, order[index], me_x)]
        return remote(
            block, block, az_send.at[kind, 1 + index], az_recv.at[kind, slot], {"z": target}
        )

    def a_z_next(kind, index):
        @pl.when(inner)
        def _():
            a_z(kind, index).start()

    def a_z_done(kind):
        @pl.when(last_z == 0)
        def _():
            a_z_own(kind, 1).wait_send()

        @pl.when(first_z == 0)
        def _():
            a_z_own(kind, 0).wait_send()

        @pl.when(inner)
        def _():
            for index in range(1, z_size):
                a_z(kind, index).wait_send()

    def a_z_in(kind, step):
        block = bufs[kind].at[block_of(kind, step, me_x)]
        return remote(block, block, az_send.at[kind, 0], az_recv.at[kind, step], to_z(1))

    def a_x(kind, step):
        return remote(
            source(kind, step),
            bufs[kind].at[block_of(kind, step, me_x)],
            ax_send.at[kind, step],
            ax_recv.at[kind, step],
            to_x,
        )

    def a_x_in(kind, step):
        block = bufs[kind].at[block_of(kind, step, 1 - me_x)]
        return remote(block, block, ax_send.at[kind, step], ax_recv.at[kind, step], to_x)

    def a_c(kind, step, far):
        x_at = 1 - me_x if far else me_x
        block = bufs[kind].at[row_block(step, x_at, me_c)]
        src = source(kind, step) if kind and not far else block
        slot = step + z_size * far
        return remote(src, block, ac_send.at[kind, slot], ac_recv.at[kind, slot], to_c)

    def a_c_in(kind, step, far):
        x_at = 1 - me_x if far else me_x
        block = bufs[kind].at[row_block(step, x_at, 1 - me_c)]
        slot = step + z_size * far
        return remote(block, block, ac_send.at[kind, slot], ac_recv.at[kind, slot], to_c)

    def f_z(kind, step, act):
        target = lax.rem(me_z + step, z_size)

        def piece(index, src, dst):
            return remote(
                ffn_in[kind].at[:, src],
                w3_out.at[kind, here, dst],
                fz_send.at[kind, step, index],
                fz_recv.at[kind, step, index],
                to_z(step),
            )

        act(piece(0, *body_of(target)))

        @pl.when(is_inner(target))
        def _():
            act(piece(1, *tail_of(target)))

    def f_z_wait(kind, step):
        block = row_block(step, me_x, me_c)

        def piece(index, dst):
            part = w3_out.at[kind, block, dst]
            return remote(
                part, part, fz_send.at[kind, step, index], fz_recv.at[kind, step, index], to_z(step)
            )

        piece(0, pl.ds(0, main)).wait_recv()

        @pl.when(inner)
        def _():
            piece(1, pl.ds(main, 128)).wait_recv()

    def f_x(kind, step, x_at, act):
        for case, columns in ((inner, units), (first_z + last_z > 0, main)):

            @pl.when(case)
            def _(columns=columns):
                block = w3_out.at[kind, row_block(step, x_at, me_c), pl.ds(0, columns)]
                act(remote(block, block, fx_send.at[kind, step], fx_recv.at[kind, step], to_x))

    def f_x_start(kind, step):
        f_x(kind, step, me_x, lambda copy: copy.start())

    def f_x_wait(kind, step):
        f_x(kind, step, 1 - me_x, lambda copy: copy.wait_recv())

    def f_x_done(kind, step):
        f_x(kind, step, me_x, lambda copy: copy.wait_send())

    def f_c(kind, step, far):
        block = w3_out.at[kind, row_block(step, 1 - me_x if far else me_x, me_c)]
        slot = step + z_size * far
        return remote(block, block, fc_send.at[kind, slot], fc_recv.at[kind, slot], to_c)

    def f_c_in(kind, step, far):
        block = w3_out.at[kind, row_block(step, 1 - me_x if far else me_x, 1 - me_c)]
        slot = step + z_size * far
        return remote(block, block, fc_send.at[kind, slot], fc_recv.at[kind, slot], to_c)

    def d_source(step):
        return cot_hbm if isinstance(step, int) else dy_out.at[step, mine]

    def d_z_own(right):
        slot = 1 if right else z_size - 1
        return remote(
            cot_hbm, dy_out.at[slot, mine], dz_send.at[right], dz_recv.at[slot], to_z(slot)
        )

    def d_z_start():
        @pl.when(last_z == 0)
        def _():
            d_z_own(1).start()

        @pl.when(first_z == 0)
        def _():
            d_z_own(0).start()

    def d_z(index):
        target, slot = hops[index]
        return remote(
            dy_out.at[order[index], mine],
            dy_out.at[slot, mine],
            dz_send.at[1 + index],
            dz_recv.at[slot],
            {"z": target},
        )

    def d_z_done():
        @pl.when(last_z == 0)
        def _():
            d_z_own(1).wait_send()

        @pl.when(first_z == 0)
        def _():
            d_z_own(0).wait_send()

        @pl.when(inner)
        def _():
            for index in range(1, z_size):
                d_z(index).wait_send()

    def d_z_in(step):
        block = dy_out.at[step, mine]
        return remote(block, block, dz_send.at[0], dz_recv.at[step], to_z(1))

    def d_y(step):
        return remote(
            d_source(step), dy_out.at[step, mine], dy_send.at[step], dy_recv.at[step], to_y
        )

    def d_y_in(step):
        block = dy_out.at[step, theirs]
        return remote(block, block, dy_send.at[step], dy_recv.at[step], to_y)

    for kind in (1, 0, 2):
        a_z_start(kind)
        a_x(kind, 0).start()
    kv_y(0, 0).start()
    tok_y.start()
    for kind in (1, 2):
        a_c(kind, 0, 0).start()

    for at_end, away in ((first_z, 1), (last_z, z_size - 1)):

        @pl.when(at_end > 0)
        def _(away=away):
            for kind in range(3):
                f_z(kind, away, lambda copy: copy.start())

    tok[mine, :] = tok_ref[...]
    seq = 2 * own
    query_at = lax.broadcasted_iota(jnp.int32, (seq, seq), 0)
    key_at = lax.broadcasted_iota(jnp.int32, (seq, seq), 1)
    same = seg_ref[...].T[:, :1] == seg_ref[:1, :]
    allowed = same & (key_at <= query_at) & (query_at - key_at < WINDOW)
    allow_ref[...] = jnp.where(allowed, 1.0, 0.0)
    d_y(0).start()

    def from_x(index):
        step = order[index]
        for kind in (1, 0, 2):
            a_x_in(kind, step).wait_recv()
            if kind:
                a_c(kind, step, 1).start()
            else:
                kv_y(step, 1).start()

    def from_y(index):
        step = order[index]
        for far in range(2):
            kv_y_in(step, far).wait_recv()
            a_c(0, step, far).start()

    for index in range(1, z_size):
        step = order[index]
        for kind in (1, 0, 2):
            a_z_in(kind, step).wait_recv()
            a_z_next(kind, index)
            a_x(kind, step).start()
            if kind:
                a_c(kind, step, 0).start()
            else:
                kv_y(step, 0).start()
        if index == z_size - 2:
            d_z_start()
        if index == z_size - 1:
            for copy in own_f:
                copy.wait()

            @pl.when(inner)
            def _():
                for kind in range(3):
                    own_tail(kind).wait()

            for kind in range(3):
                for away, sent in ((1, first_z), (3, last_z), (2, 0)):

                    @pl.when(sent == 0 if away != 2 else me_z >= 0)
                    def _(kind=kind, away=away):
                        f_z(kind, away, lambda copy: copy.start())

            for kind in range(3):
                f_x_start(kind, 0)
                f_c(kind, 0, 0).start()
        if index >= 2:
            from_x(index - 2)
            from_y(index - 2)
    for index in (z_size - 2, z_size - 1):
        from_x(index)
        from_y(index)

    def hand_on(kind, step):
        f_z_wait(kind, step)
        f_x_start(kind, step)
        f_c(kind, step, 0).start()

    def cross(kind, step):
        f_x_wait(kind, step)
        f_c(kind, step, 1).start()

    def pass_cotangent(step):
        d_z_in(order[step]).wait_recv()

        @pl.when(inner)
        def _():
            d_z(step).start()

        d_y(order[step]).start()

    def pass_if(case, step):
        @pl.when(case)
        def _():
            pass_cotangent(step)

    outer = first_z + last_z > 0
    tok_y_in.wait_recv()
    own_q.wait()
    own_o.wait()
    for kind in (0, 1):
        for step in range(z_size):
            for far in range(2):
                a_c_in(kind, step, far).wait_recv()

    gains = kv_w[:, 2 * head :].astype(jnp.float32).T[:8, :]
    gain_ref[...] = gains

    def norm_rows(index, carry):
        at = pl.ds(pl.multiple_of(index * 32, 32), 32)
        values = tok[at, :].astype(jnp.float32)
        scale = lax.rsqrt(jnp.mean(values * values, axis=-1, keepdims=True) + epsilon)
        n1_ref[at, :] = (values * scale * gain_ref[0:1, :]).astype(jnp.bfloat16)
        return carry

    lax.fori_loop(0, 2 * own // 32, norm_rows, 0)
    hand_on(0, order[1])
    table = (table_ref[0], table_ref[1])
    key_ref[...] = spin(dot_nn(n1_ref[...], kv_w[:, :head]), table).astype(jnp.bfloat16)
    val_ref[...] = dot_nn(n1_ref[...], kv_w[:, head : 2 * head]).astype(jnp.bfloat16)
    hand_on(0, order[2])
    head_scale = head ** (-0.5)
    heads = att_ref.shape[1] // head

    half_cols = att_ref.shape[1] // 2
    for index in range(2):
        cols = pl.ds(index * half_cols, half_cols)
        query[:, cols] = dot_nn(n1_ref[...], q_w[:, cols])

    def attend(index):
        cols = pl.ds(index * head, head)
        rotated = (spin(query[:, cols], table) * head_scale).astype(jnp.bfloat16)
        rot_ref[:, cols] = rotated
        probs = head_probs(rotated, key_ref[...], allow_ref[...]).astype(jnp.bfloat16)
        att_ref[:, cols] = dot_nn(probs, val_ref[...]).astype(jnp.bfloat16)

    tasks = [
        lambda: (pass_cotangent(1), pass_if(inner, 2)),
        lambda: hand_on(0, order[3]),
        lambda: (cross(0, 0), hand_on(1, order[1])),
        lambda: cross(1, 0),
        lambda: (cross(2, 0), hand_on(1, order[2])),
    ]
    for index in range(heads):
        attend(index)
        if index < len(tasks):
            tasks[index]()
    for step in range(z_size):
        for far in range(2):
            a_c_in(2, step, far).wait_recv()
    saves = [
        local(kv_w, kv_out),
        local(q_w, wq_out),
        local(o_w, wo_out),
    ]
    span = width // 4

    def project(index, carry):
        cols = pl.ds(pl.multiple_of(index * span, span), span)
        part[:, cols] = matmul_nt(att_ref[...], o_w[cols, :]).astype(jnp.bfloat16)
        return carry

    lax.fori_loop(0, 4, project, 0)
    part_out.start()
    hand_on(1, order[3])
    pass_if(outer, 2)
    pass_if(inner, 3)
    cross(0, order[1])
    hand_on(2, order[1])
    part_out.wait_recv()

    def middle(index, carry):
        at = pl.ds(pl.multiple_of(index * 32, 32), 32)
        there = pl.ds(pl.multiple_of(me_y * own + index * 32, 32), 32)
        values = (
            tok_ref[at, :].astype(jnp.float32)
            + part[there, :].astype(jnp.float32)
            + part_y[at, :].astype(jnp.float32)
        )
        mid_ref[at, :] = values
        scale = lax.rsqrt(jnp.mean(values * values, axis=-1, keepdims=True) + epsilon)
        n2_ref[there, :] = (values * scale * gain_ref[1:2, :]).astype(jnp.bfloat16)
        return carry

    lax.fori_loop(0, own // 32, middle, 0)
    n2_y.start()
    hand_on(2, order[2])
    cross(0, order[2])
    cross(0, order[3])
    hand_on(2, order[3])
    pass_if(outer, 3)
    for kind in (1, 2):
        for index in (1, 2, 3):
            cross(kind, order[index])
    for kind in range(3):
        for step in range(z_size):
            for far in range(2):
                f_c_in(kind, step, far).wait_recv()
    for step in range(z_size):
        d_y_in(step).wait_recv()
    n2_y_in.wait_recv()

    for kind in range(3):
        a_z_done(kind)
    d_z_done()
    tok_y.wait_send()
    part_out.wait_send()
    n2_y.wait_send()
    own_d.wait()
    for copy in saves:
        copy.wait()
    for step in range(z_size):
        d_y(step).wait_send()
        for far in range(2):
            kv_y(step, far).wait_send()
        for kind in range(3):
            if step:
                f_z(kind, step, lambda copy: copy.wait_send())
            a_x(kind, step).wait_send()
            f_x_done(kind, step)
            for far in range(2):
                a_c(kind, step, far).wait_send()
                f_c(kind, step, far).wait_send()


def pre_call(tokens, w_kv, gains, table, segments, cotangent, w_query, w_out, ffn):
    z_size = lax.axis_size("z")
    own, width = tokens.shape
    seq = 2 * own
    rows, cols = w_query.shape
    head = table.shape[2] * 2
    units = ragged_split(ffn[0].shape[1], z_size)[1]
    low = lambda *dims: jax.ShapeDtypeStruct(dims, jnp.bfloat16)
    full = lambda *dims: jax.ShapeDtypeStruct(dims, jnp.float32)
    dma = lambda *lead: pltpu.SemaphoreType.DMA(lead)
    vmem = pl.BlockSpec(memory_space=pltpu.VMEM)
    hbm = pl.BlockSpec(memory_space=pl.ANY)
    wide = lambda *lead: pltpu.VMEM((*lead, width), jnp.bfloat16)
    return pl.pallas_call(
        functools.partial(pre_kernel, z_size),
        out_shape=(
            low(seq, width),
            low(seq, cols),
            low(seq, head),
            low(seq, head),
            low(seq, cols),
            full(own, width),
            low(seq, width),
            full(8, width),
            full(seq, seq),
            low(width, 2 * head + 128),
            low(width, cols),
            low(width, cols),
            low(3, width, units),
            low(z_size, seq, width),
        ),
        in_specs=[vmem] * 5 + [hbm] * 6,
        out_specs=(vmem,) * 9 + (hbm,) * 5,
        scratch_shapes=[
            pltpu.VMEM((width, 2 * head + 128), jnp.bfloat16),
            pltpu.VMEM((width, cols), jnp.bfloat16),
            pltpu.VMEM((width, cols), jnp.bfloat16),
            wide(seq),
            wide(seq),
            wide(own),
            pltpu.VMEM((seq, cols), jnp.float32),
            dma(4),
            dma(4),
            dma(2 * z_size),
            dma(2 * z_size),
            dma(3, z_size + 1),
            dma(3, z_size),
            dma(3, z_size),
            dma(3, z_size),
            dma(3, 2 * z_size),
            dma(3, 2 * z_size),
            dma(3, z_size, 2),
            dma(3, z_size, 2),
            dma(3, z_size),
            dma(3, z_size),
            dma(3, 2 * z_size),
            dma(3, 2 * z_size),
            dma(z_size + 1),
            dma(z_size),
            dma(z_size),
            dma(z_size),
            dma(16),
        ],
        compiler_params=pltpu.CompilerParams(
            collective_id=1, has_side_effects=True, vmem_limit_bytes=VMEM_BYTES
        ),
        cost_estimate=pl.CostEstimate(
            flops=8 * seq * width * cols,
            bytes_accessed=8 * width * (cols + units),
            transcendentals=seq * seq * cols // head,
        ),
    )(tokens, w_kv, gains, table, segments, cotangent, w_query, w_out, *ffn)


def post_kernel(
    z_size,
    main,
    tok_ref,
    gain_ref,
    gain_part_ref,
    n1_ref,
    rot_ref,
    key_ref,
    val_ref,
    att_ref,
    table_ref,
    allow_ref,
    kv_hbm,
    wq_hbm,
    wo_hbm,
    mix_hbm,
    gmf_hbm,
    gmb_hbm,
    mid_hbm,
    sums_hbm,
    mixed_ref,
    tgrad_ref,
    gsum_ref,
    kvg_ref,
    qg_ref,
    og_ref,
    ffn_out,
    kv_w,
    q_w,
    o_w,
    o_part,
    gm,
    gm_f,
    gq,
    gkv,
    kv_sum,
    back_y,
    mix_y,
    mix_z,
    mix_s,
    o_c,
    o_x,
    o_z,
    q_c,
    q_x,
    q_z,
    kv_y,
    kv_c,
    kv_x,
    kv_z,
    gain_own,
    gain_in,
    ffn_in,
    ffn_own,
    load_sem,
    own_sem,
    fx_send,
    fx_recv,
    fz_send,
    fz_recv,
    y_send,
    y_recv,
    my_send,
    my_recv,
    mz_send,
    mz_recv,
    wc_send,
    wc_recv,
    wx_send,
    wx_recv,
    wz_send,
    wz_recv,
    kc_send,
    kc_recv,
    kz_send,
    kz_recv,
    g_send,
    g_recv,
):
    me_z, me_x = lax.axis_index("z"), lax.axis_index("x")
    me_c, me_y = lax.axis_index("c"), lax.axis_index("mp")
    own, width = tok_ref.shape
    seq = 2 * own
    head = key_ref.shape[1]
    cols_here = att_ref.shape[1]
    heads = cols_here // head
    rows = qg_ref.shape[0]
    span = width // z_size
    mine = pl.ds(pl.multiple_of(me_y * own, own), own)
    theirs = pl.ds(pl.multiple_of((1 - me_y) * own, own), own)
    to_y, to_x, to_c = {"mp": 1 - me_y}, {"x": 1 - me_x}, {"c": 1 - me_c}
    head_scale = head ** (-0.5)

    def behind(step):
        return lax.rem(me_z - step + z_size, z_size)

    def to_z(step):
        return {"z": lax.rem(me_z + step, z_size)}

    def row_block(step, x_at, c_at):
        start = ((behind(step) * 2 + x_at) * 2 + c_at) * rows
        return pl.ds(pl.multiple_of(start, rows), rows)

    loads = [
        pltpu.make_async_copy(wo_hbm, o_w, load_sem.at[0]),
        pltpu.make_async_copy(wq_hbm, q_w, load_sem.at[1]),
        pltpu.make_async_copy(
            kv_hbm.at[:, :, :, :, :, pl.ds(0, 2 * head)], kv_w, load_sem.at[2]
        ),
    ]
    for step in range(z_size):
        loads.append(
            pltpu.make_async_copy(mix_hbm.at[step, me_y], mix_s.at[step], load_sem.at[3 + step])
        )
    loads.append(pltpu.make_async_copy(gmf_hbm, gm_f, load_sem.at[3 + z_size]))
    loads.append(pltpu.make_async_copy(gmb_hbm, gm.at[mine], load_sem.at[4 + z_size]))
    mid_load = pltpu.make_async_copy(mid_hbm, gm_f, load_sem.at[5 + z_size])
    for load in loads:
        load.start()

    barrier = pltpu.get_barrier_semaphore()
    peers = [to_y, to_x, to_c] + [to_z(step) for step in range(1, z_size)]
    for where in peers:
        pl.semaphore_signal(barrier, inc=1, device_id=where, device_id_type=MESH_ID)
    pl.semaphore_wait(barrier, len(peers))

    tasks = [(step, kind) for step in (2, 3) for kind in range(3)]

    def f_x(index):
        step, kind = tasks[index]
        return remote(
            sums_hbm.at[kind, step, 1],
            ffn_in.at[index],
            fx_send.at[index],
            fx_recv.at[index],
            to_x,
        )

    def f_own(index):
        step, kind = tasks[index]
        return pltpu.make_async_copy(
            sums_hbm.at[kind, step, 0], ffn_own.at[index % 2], own_sem.at[index % 2]
        )

    def f_z(step, kind, source_z, act):
        for case, columns in (
            ((source_z > 0) & (source_z < z_size - 1), ffn_out.shape[3]),
            ((source_z == 0) | (source_z == z_size - 1), main),
        ):

            @pl.when(case)
            def _(columns=columns):
                cols = pl.ds(0, columns)
                if step == 1:
                    src = sums_hbm.at[kind, 1, 0, :, cols]
                else:
                    src = ffn_in.at[tasks.index((step, kind)), :, cols]
                act(
                    remote(
                        src,
                        ffn_out.at[kind, step, :, cols],
                        fz_send.at[kind, step],
                        fz_recv.at[kind, step],
                        to_z(step),
                    )
                )

    def tick(index):
        step, kind = tasks[index]
        f_x(index).wait_recv()
        f_own(index).wait()
        block = ffn_in.at[index]
        add_rows(block, [ffn_own.at[index % 2]], block, rows)
        if index + 2 < len(tasks):
            f_own(index + 2).start()
        f_z(step, kind, me_z, lambda copy: copy.start())

    def f_x_own(kind):
        return remote(
            sums_hbm.at[kind, 0, 1],
            ffn_out.at[kind, 0],
            fx_send.at[len(tasks) + kind],
            fx_recv.at[len(tasks) + kind],
            to_x,
        )

    f_own(0).start()
    f_own(1).start()
    for index in range(len(tasks)):
        f_x(index).start()
    for kind in range(3):
        f_z(1, kind, me_z, lambda copy: copy.start())

    gm_y = remote(gmb_hbm, gm.at[mine], y_send.at[0], y_recv.at[0], to_y)
    gm_y_in = remote(gm.at[theirs], gm.at[theirs], y_send.at[0], y_recv.at[0], to_y)
    gm_y.start()

    first_z, last_z = (z_size - 1 - me_z) // (z_size - 1), me_z // (z_size - 1)
    inner = first_z + last_z == 0
    order = (
        0,
        1 + (me_z + 1) // 2,
        2 + (2 * me_z - 3) * (1 - first_z - last_z),
        3 - 2 * (me_z // 2),
    )
    right = (None, 1 - me_z // 2, (3 - me_z) * (2 - me_z) // 6 + me_z // 2 * (1 - last_z), 1 - me_z // 2)

    def hop_slot(index):
        step, way = order[index], right[index]
        return way * lax.rem(step + 1, z_size) + (1 - way) * (step - 1 + 4 * ((3 - step) // 2))

    def hop_target(index):
        return {"z": me_z + 2 * right[index] - 1}

    def mix_over_y(step):
        return remote(
            mix_hbm.at[step, 1 - me_y], mix_y.at[step], my_send.at[step], my_recv.at[step], to_y
        )

    def mix_over_z(index):
        slot = hop_slot(index)
        return remote(
            mix_s.at[order[index]],
            mix_z.at[slot],
            mz_send.at[index],
            mz_recv.at[slot],
            hop_target(index),
        )

    def mix_z_in(slot):
        return remote(mix_z.at[slot], mix_z.at[slot], mz_send.at[1], mz_recv.at[slot], to_z(1))

    def mix_add(step, others, last):
        def add_tile(tile, carry):
            at = pl.ds(pl.multiple_of(tile * TILE, TILE), TILE)
            total = mix_s[step, at, :].astype(jnp.float32)
            for other in others:
                total = total + other[at, :].astype(jnp.float32)
            if last:
                mixed_ref[:, at] = (gm_f[:, at] + total.T).astype(jnp.bfloat16)
            else:
                mix_s[step, at, :] = total.astype(jnp.bfloat16)
            return carry

        lax.fori_loop(0, width // TILE, add_tile, 0)

    def mix_step(index):
        step = order[index]
        mix_over_y(step).wait_recv()
        from_y = mix_y.at[step]
        if index:

            @pl.when(inner)
            def _():
                mix_z_in(step).wait_recv()
                mix_add(step, [from_y, mix_z.at[step]], False)

            @pl.when(first_z + last_z > 0)
            def _():
                mix_add(step, [from_y], False)

            mix_over_z(index).start()
        else:
            mid_load.wait()

            @pl.when(first_z == 0)
            def _():
                mix_z_in(0).wait_recv()

            @pl.when(last_z == 0)
            def _():
                mix_z_in(z_size).wait_recv()

            @pl.when(inner)
            def _():
                mix_add(0, [from_y, mix_z.at[0], mix_z.at[z_size]], True)

            @pl.when(first_z > 0)
            def _():
                mix_add(0, [from_y, mix_z.at[z_size]], True)

            @pl.when(last_z > 0)
            def _():
                mix_add(0, [from_y, mix_z.at[0]], True)

    for index in (1, 2, 3, 0):
        mix_over_y(order[index]).start()

    kinds = ((o_part, o_c, o_x, o_z, og_ref), (o_w, q_c, q_x, q_z, qg_ref))

    def w_c(kind, step, far):
        x_at = 1 - me_x if far else me_x
        return remote(
            kinds[kind][0].at[row_block(step, x_at, 1 - me_c)],
            kinds[kind][1].at[step, far],
            wc_send.at[kind, step, far],
            wc_recv.at[kind, step, far],
            to_c,
        )

    def w_x(kind, step):
        return remote(
            kinds[kind][0].at[row_block(step, 1 - me_x, me_c)],
            kinds[kind][2].at[step],
            wx_send.at[kind, step],
            wx_recv.at[kind, step],
            to_x,
        )

    def w_z(kind, index):
        step, slot = order[index], hop_slot(index)
        return remote(
            kinds[kind][0].at[row_block(step, me_x, me_c)],
            kinds[kind][3].at[slot],
            wz_send.at[kind, index],
            wz_recv.at[kind, slot],
            hop_target(index),
        )

    def w_z_in(kind, slot):
        block = kinds[kind][3].at[slot]
        return remote(block, block, wz_send.at[kind, 1], wz_recv.at[kind, slot], to_z(1))

    def w_x_stage(kind, index):
        step = order[index]
        w_c(kind, step, 1).wait_recv()
        block = kinds[kind][0].at[row_block(step, 1 - me_x, me_c)]
        add_rows(block, [kinds[kind][1].at[step, 1]], block, rows)
        w_x(kind, step).start()

    def w_z_stage(kind, index):
        part, from_c, from_x, from_z, result = kinds[kind]
        step = order[index]
        w_c(kind, step, 0).wait_recv()
        w_x(kind, step).wait_recv()
        block = part.at[row_block(step, me_x, me_c)]
        others = [from_c.at[step, 0], from_x.at[step]]
        if index:

            @pl.when(inner)
            def _():
                w_z_in(kind, step).wait_recv()
                add_rows(block, [*others, from_z.at[step]], block, rows)

            @pl.when(first_z + last_z > 0)
            def _():
                add_rows(block, others, block, rows)

            w_z(kind, index).start()
        else:

            @pl.when(first_z == 0)
            def _():
                w_z_in(kind, 0).wait_recv()

            @pl.when(last_z == 0)
            def _():
                w_z_in(kind, z_size).wait_recv()

            @pl.when(inner)
            def _():
                add_rows(block, [*others, from_z.at[0], from_z.at[z_size]], result, rows)

            @pl.when(first_z > 0)
            def _():
                add_rows(block, [*others, from_z.at[z_size]], result, rows)

            @pl.when(last_z > 0)
            def _():
                add_rows(block, [*others, from_z.at[0]], result, rows)

    def w_product(kind, index, left, values):
        step = order[index]
        at = pl.ds(pl.multiple_of(behind(step) * span, 128), span)
        turned = left[:, at].T

        def tile_body(tile, carry):
            cols = pl.ds(pl.multiple_of(tile * TILE, TILE), TILE)
            kinds[kind][0][at, cols] = dot_nn(turned, values[:, cols]).astype(jnp.bfloat16)
            return carry

        lax.fori_loop(0, cols_here // TILE, tile_body, 0)
        for far in (1, 0):
            w_c(kind, step, far).start()

    tick(0)
    tick(1)
    loads[-1].wait()
    gm_y_in.wait_recv()
    w_product(0, 1, gm, att_ref)
    w_product(0, 2, gm, att_ref)
    w_x_stage(0, 1)
    w_product(0, 3, gm, att_ref)
    w_x_stage(0, 2)
    tick(2)
    w_product(0, 0, gm, att_ref)
    w_x_stage(0, 3)
    for load in loads[:-1]:
        load.wait()

    kv_sum[...] = jnp.zeros(kv_sum.shape, jnp.float32)
    table = (table_ref[0], table_ref[1])

    for index in range(2):
        cols = pl.ds(index * (cols_here // 2), cols_here // 2)
        gq[:, cols] = dot_nn(gm[...], o_w[:, cols]).astype(jnp.bfloat16)

    def attend_back(index):
        cols = pl.ds(index * head, head)
        grad_vals = gq[:, cols]
        rotated = rot_ref[:, cols]
        probs = head_probs(rotated, key_ref[...], allow_ref[...])
        grad_probs = matmul_nt(grad_vals, val_ref[...])
        delta = jnp.sum(probs * grad_probs, axis=-1, keepdims=True)
        grad_scores = (probs * (grad_probs - delta)).astype(jnp.bfloat16)
        grad_rot = dot_nn(grad_scores, key_ref[...])
        gq[:, cols] = (spin_back(grad_rot, table) * head_scale).astype(jnp.bfloat16)
        kv_sum[0] += matmul_tn(grad_scores, rotated)
        kv_sum[1] += matmul_tn(probs.astype(jnp.bfloat16), grad_vals)

    for index in range(heads):
        attend_back(index)
        if index == 0:
            w_x_stage(0, 0)
        if 3 + index < len(tasks):
            tick(3 + index)
        if index == heads - 1:
            mix_step(1)
    gkv[:, :head] = spin_back(kv_sum[0], table).astype(jnp.bfloat16)
    gkv[:, head:] = kv_sum[1].astype(jnp.bfloat16)

    w_product(1, 1, n1_ref, gq)
    w_product(1, 2, n1_ref, gq)
    w_x_stage(1, 1)
    w_z_stage(0, 1)
    w_product(1, 3, n1_ref, gq)
    w_x_stage(1, 2)
    w_product(1, 0, n1_ref, gq)
    w_x_stage(1, 3)
    w_x_stage(1, 0)
    for kind in range(3):
        f_x_own(kind).start()

    gm_y.wait_send()
    back = gm
    def input_tile(index, carry):
        at = pl.ds(pl.multiple_of(index * span, 128), span)
        back[:, at] = (
            matmul_nt(gq[...], q_w[at, :]) + matmul_nt(gkv[...], kv_w[index].reshape(span, 2 * head))
        ).astype(jnp.bfloat16)
        return carry

    lax.fori_loop(0, z_size, input_tile, 0)
    back_out = remote(back.at[theirs], back_y, y_send.at[1], y_recv.at[1], to_y)
    back_out.start()

    kv_part = kv_w

    def kv_tile(index, carry):
        at = pl.ds(pl.multiple_of(index * span, 128), span)
        product = dot_nn(n1_ref[:, at].T, gkv[...]).astype(jnp.bfloat16)
        kv_part[index] = product.reshape(kv_part.shape[1:])
        return carry

    lax.fori_loop(0, z_size, kv_tile, 0)
    kv_over_y = remote(kv_part.at[:, :, :, 1 - me_y], kv_y, y_send.at[2], y_recv.at[2], to_y)
    kv_over_y.start()
    mix_step(2)
    w_z_stage(0, 2)
    mix_step(3)
    w_z_stage(0, 3)

    back_out.wait_recv()

    def input_rows(index, total):
        at = pl.ds(pl.multiple_of(index * 32, 32), 32)
        there = pl.ds(pl.multiple_of(me_y * own + index * 32, 32), 32)
        upstream = back[there, :].astype(jnp.float32) + back_y[at, :].astype(jnp.float32)
        grad, gain_part = norm_back(
            tok_ref[at, :].astype(jnp.float32), gain_ref[0:1, :], upstream
        )
        tgrad_ref[at, :] = (gm_f[at, :] + grad).astype(jnp.bfloat16)
        return total + gain_part

    attn_gain_part = lax.fori_loop(
        0, own // 32, input_rows, jnp.zeros((1, width), jnp.float32)
    )
    for index in range(4):
        at = slice(index * span, (index + 1) * span)
        gain_own[0, index : index + 1, :] = attn_gain_part[:, at]
        gain_own[0, 4 + index : 5 + index, :] = gain_part_ref[4 + index : 5 + index, :]

    def gain_send(stage, where):
        return remote(
            gain_own.at[stage], gain_in.at[stage], g_send.at[stage], g_recv.at[stage], where
        )

    gain_hops = [gain_send(0, to_y), gain_send(1, to_c), gain_send(2, to_x)]
    gain_last = [
        remote(
            gain_own.at[3], gain_in.at[2 + step], g_send.at[2 + step], g_recv.at[2 + step], to_z(step)
        )
        for step in range(1, z_size)
    ]

    def gain_fold(stage):
        gain_hops[stage].wait_recv()
        gain_own[stage + 1] = gain_own[stage] + gain_in[stage]

    gain_hops[0].start()
    mid_load.start()
    w_z_stage(1, 1)
    w_z_stage(0, 0)
    w_z_stage(1, 2)
    gain_fold(0)
    gain_hops[1].start()
    mix_step(0)
    w_z_stage(1, 3)
    gain_fold(1)
    gain_hops[2].start()
    kv_over_y.wait_recv()

    def kv_add_y(index, carry):
        for x_at in range(2):
            for c_at in range(2):
                block = kv_part.at[index, x_at, c_at, me_y]
                block[...] = (
                    block[...].astype(jnp.float32) + kv_y[index, x_at, c_at].astype(jnp.float32)
                ).astype(jnp.bfloat16)
        return carry

    lax.fori_loop(0, z_size, kv_add_y, 0)
    kv_over_c = remote(
        kv_part.at[:, :, 1 - me_c, me_y], kv_c, kc_send.at[0], kc_recv.at[0], to_c
    )
    kv_over_c.start()
    gain_fold(2)
    for copy in gain_last:
        copy.start()
    kv_over_c.wait_recv()

    def kv_add_c(index, carry):
        for x_at in range(2):
            block = kv_part.at[index, x_at, me_c, me_y]
            block[...] = (
                block[...].astype(jnp.float32) + kv_c[index, x_at].astype(jnp.float32)
            ).astype(jnp.bfloat16)
        return carry

    lax.fori_loop(0, z_size, kv_add_c, 0)
    kv_over_x = remote(
        kv_part.at[:, 1 - me_x, me_c, me_y], kv_x, kc_send.at[1], kc_recv.at[1], to_x
    )
    kv_over_x.start()
    w_z_stage(1, 0)
    kv_over_x.wait_recv()

    def kv_add_x(index, carry):
        block = kv_part.at[index, me_x, me_c, me_y]
        block[...] = (
            block[...].astype(jnp.float32) + kv_x[index].astype(jnp.float32)
        ).astype(jnp.bfloat16)
        return carry

    lax.fori_loop(0, z_size, kv_add_x, 0)
    kv_over_z = [
        remote(
            kv_part.at[lax.rem(me_z + step, z_size), me_x, me_c, me_y],
            kv_z.at[step - 1],
            kz_send.at[step],
            kz_recv.at[step],
            to_z(step),
        )
        for step in range(1, z_size)
    ]
    for copy in kv_over_z:
        copy.start()
    for copy in gain_last:
        copy.wait_recv()
    gsum_ref[...] = gain_own[3] + gain_in[3] + gain_in[4] + gain_in[5]
    for copy in kv_over_z:
        copy.wait_recv()
    kvg_ref[...] = (
        kv_part[me_z, me_x, me_c, me_y].astype(jnp.float32)
        + kv_z[0].astype(jnp.float32)
        + kv_z[1].astype(jnp.float32)
        + kv_z[2].astype(jnp.float32)
    )

    back_out.wait_send()
    kv_over_y.wait_send()
    kv_over_c.wait_send()
    kv_over_x.wait_send()
    for kind in range(3):
        f_x_own(kind).wait()
    for index in range(len(tasks)):
        f_x(index).wait_send()
    for step in range(1, z_size):
        for kind in range(3):
            f_z(step, kind, me_z, lambda copy: copy.wait_send())
            f_z(step, kind, behind(step), lambda copy: copy.wait_recv())
    for copy in gain_hops + gain_last + kv_over_z:
        copy.wait_send()
    for step in range(z_size):
        mix_over_y(step).wait_send()
        if step:
            mix_over_z(step).wait_send()
        for kind in range(2):
            w_c(kind, step, 0).wait_send()
            w_c(kind, step, 1).wait_send()
            w_x(kind, step).wait_send()
            if step:
                w_z(kind, step).wait_send()


def post_call(
    tokens,
    gains,
    gain_part,
    normed_one,
    rotated,
    keys,
    values,
    attn_vals,
    table,
    allowed,
    kv_weight,
    query_weight,
    out_weight,
    mix_parts,
    grad_mid,
    grad_mid_low,
    mid,
    ffn_sums,
    main,
):
    z_size = lax.axis_size("z")
    own, width = tokens.shape
    seq = 2 * own
    head = keys.shape[1]
    cols = attn_vals.shape[1]
    rows = width // (4 * z_size)
    units = ffn_sums.shape[4]
    low = lambda *dims: pltpu.VMEM(dims, jnp.bfloat16)
    full = lambda *dims: pltpu.VMEM(dims, jnp.float32)
    out_full = lambda *dims: jax.ShapeDtypeStruct(dims, jnp.float32)
    out_low = lambda *dims: jax.ShapeDtypeStruct(dims, jnp.bfloat16)
    dma = lambda *lead: pltpu.SemaphoreType.DMA(lead)
    vmem = pl.BlockSpec(memory_space=pltpu.VMEM)
    hbm = pl.BlockSpec(memory_space=pl.ANY)
    z = z_size
    return pl.pallas_call(
        functools.partial(post_kernel, z_size, main),
        out_shape=(
            out_low(own, width),
            out_low(own, width),
            out_full(8, width // z),
            out_full(rows // 2, 2 * head),
            out_full(rows, cols),
            out_full(rows, cols),
            out_low(3, z, rows, units),
        ),
        in_specs=[vmem] * 10 + [hbm] * 8,
        out_specs=(vmem,) * 6 + (hbm,),
        scratch_shapes=[
            low(z, 2, 2, 2, rows // 2, 2 * head),
            low(width, cols),
            low(width, cols),
            low(width, cols),
            low(seq, width),
            full(own, width),
            low(seq, cols),
            low(seq, 2 * head),
            full(2, seq, head),
            low(own, width),
            low(z, width, own),
            low(z + 1, width, own),
            low(z, width, own),
            low(z, 2, rows, cols),
            low(z, rows, cols),
            low(z + 1, rows, cols),
            low(z, 2, rows, cols),
            low(z, rows, cols),
            low(z + 1, rows, cols),
            low(z, 2, 2, rows // 2, 2 * head),
            low(z, 2, rows // 2, 2 * head),
            low(z, rows // 2, 2 * head),
            low(z - 1, rows // 2, 2 * head),
            full(4, 8, width // z),
            full(6, 8, width // z),
            low(6, rows, units),
            low(2, rows, units),
            dma(6 + z),
            dma(2),
            dma(9),
            dma(9),
            dma(3, z),
            dma(3, z),
            dma(3),
            dma(3),
            dma(z),
            dma(z),
            dma(z),
            dma(z + 1),
            dma(2, z, 2),
            dma(2, z, 2),
            dma(2, z),
            dma(2, z),
            dma(2, z),
            dma(2, z + 1),
            dma(2),
            dma(2),
            dma(z),
            dma(z),
            dma(6),
            dma(6),
        ],
        compiler_params=pltpu.CompilerParams(
            collective_id=2, has_side_effects=True, vmem_limit_bytes=VMEM_BYTES
        ),
        cost_estimate=pl.CostEstimate(
            flops=14 * seq * width * cols,
            bytes_accessed=10 * width * cols,
            transcendentals=seq * seq * cols // head,
        ),
    )(
        tokens,
        gains,
        gain_part,
        normed_one,
        rotated,
        keys,
        values,
        attn_vals,
        table,
        allowed,
        kv_weight.reshape(z, 2, 2, 2, rows // 2, kv_weight.shape[1]),
        query_weight,
        out_weight,
        mix_parts,
        grad_mid,
        grad_mid_low,
        mid,
        ffn_sums,
    )


def layout_kernel(
    z_size,
    main,
    sum_ref,
    ffn_ref,
    q_ref,
    o_ref,
    kv_ref,
    mixed_in,
    tgrad_in,
    wg_ref,
    wu_ref,
    wd_ref,
    qg_ref,
    og_ref,
    kvg_ref,
    mixed_ref,
    tgrad_ref,
):
    me_z = lax.axis_index("z")
    for kind, out in enumerate((wg_ref, wu_ref, wd_ref)):
        for step in range(z_size):
            at = lax.rem(me_z - step + z_size, z_size)
            values = ffn_ref[kind, step].astype(jnp.float32)
            if step == 0:
                values = values + sum_ref[kind, 0, 0].astype(jnp.float32)
            body = pl.ds(pl.multiple_of(at * main, 128), main)
            out[:, body] = values[:, :main]

            @pl.when((at > 0) & (at < z_size - 1))
            def _(out=out, at=at, values=values):
                tail = z_size * main + lax.rem(at + 1, 2) * 128
                out[:, pl.ds(pl.multiple_of(tail, 128), 128)] = values[:, main:]
    qg_ref[...] = q_ref[...]
    og_ref[...] = o_ref[...]
    kvg_ref[...] = kv_ref[...]
    mixed_ref[...] = mixed_in[...]
    tgrad_ref[...] = tgrad_in[...]


def layout_call(ffn_sums, ffn_grads, query_grad, out_grad, kv_grad, mixed, tokens_grad, ffn_cols):
    z_size = lax.axis_size("z")
    main, units = ragged_split(ffn_cols, z_size)
    rows, cols = query_grad.shape
    parts = rows // 32
    kv_rows = kv_grad.shape[0] // parts
    full = lambda *dims: jax.ShapeDtypeStruct(dims, jnp.float32)
    row = lambda height, width: pl.BlockSpec((height, width), lambda index: (index, 0))
    own, width = mixed.shape
    share = pl.BlockSpec((own, width // parts), lambda index: (0, index))
    specs = [row(32, cols), row(32, cols), row(kv_rows, kv_grad.shape[1]), share, share]
    return pl.pallas_call(
        functools.partial(layout_kernel, z_size, main),
        grid=(parts,),
        out_shape=(
            *[full(rows, ffn_cols)] * 3,
            full(rows, cols),
            full(rows, cols),
            full(*kv_grad.shape),
            jax.ShapeDtypeStruct(mixed.shape, jnp.bfloat16),
            jax.ShapeDtypeStruct(mixed.shape, jnp.bfloat16),
        ),
        in_specs=[
            pl.BlockSpec((3, 1, 1, 32, units), lambda index: (0, 0, 0, index, 0)),
            pl.BlockSpec((3, z_size, 32, units), lambda index: (0, 0, index, 0)),
            *specs,
        ],
        out_specs=(*[row(32, ffn_cols)] * 3, *specs),
        compiler_params=pltpu.CompilerParams(vmem_limit_bytes=VMEM_BYTES),
    )(ffn_sums, ffn_grads, query_grad, out_grad, kv_grad, mixed, tokens_grad)


FF_SPLIT = 4


def ffn_pass(normed, grad_out, gate_weight, up_weight, down_weight):
    gate = jnp.dot(normed, gate_weight, preferred_element_type=jnp.float32)
    up_proj = jnp.dot(normed, up_weight, preferred_element_type=jnp.float32)
    grad_hidden = jnp.dot(grad_out, down_weight, preferred_element_type=jnp.float32)
    product, pull = jax.vjp(gelu_product, gate, up_proj)
    hidden = product.astype(jnp.bfloat16)
    grad_gate_f, grad_up_f = pull(grad_hidden)
    grad_gate = grad_gate_f.astype(jnp.bfloat16)
    grad_up = grad_up_f.astype(jnp.bfloat16)
    mixed_part = matmul_nt(hidden, down_weight).astype(jnp.bfloat16)
    normed_part = (matmul_nt(grad_gate, gate_weight) + matmul_nt(grad_up, up_weight)).astype(
        jnp.bfloat16
    )
    weight_parts = [
        matmul_tn(normed, grad_gate).astype(jnp.bfloat16),
        matmul_tn(normed, grad_up).astype(jnp.bfloat16),
        matmul_tn(grad_out, hidden).astype(jnp.bfloat16),
    ]
    return mixed_part, normed_part, weight_parts


def shards_general(
    tokens,
    segments,
    positions,
    cotangent,
    attn_gain,
    ffn_gain,
    w_kv,
    w_query,
    w_out,
    w_gate,
    w_up,
    w_down,
):
    everywhere = ("z", "xc", "mp")
    dp = ("z", "xc")
    z_size = lax.axis_size("z")
    xc_size = lax.axis_size("xc")
    gains = lax.all_gather(
        jnp.stack([attn_gain, ffn_gain], axis=1), everywhere, axis=0, tiled=True
    ).astype(jnp.float32)
    gain_one, gain_two = gains[:, 0], gains[:, 1]
    kv_weight = lax.all_gather(w_kv, everywhere, axis=0, tiled=True)
    head_dim = kv_weight.shape[1] // 2
    width = tokens.shape[1]
    seq_len = segments.shape[0]
    heads_here = w_query.shape[1] // head_dim
    scale = head_dim ** (-0.5)
    cosine, sine = rotary_angles(positions, head_dim)
    inputs_f = tokens.astype(jnp.float32)
    tokens_all = lax.all_gather(tokens, "mp", axis=0, tiled=True)
    normed_one = norm_gain(tokens_all.astype(jnp.float32), gain_one).astype(jnp.bfloat16)
    query_weight = lax.all_gather(w_query, dp, axis=0, tiled=True)
    out_weight = lax.all_gather(w_out, dp, axis=0, tiled=True)

    rows = w_gate.shape[0]
    unit = w_gate.shape[1] // z_size

    def spread(weight):
        pieces = weight.reshape(rows, z_size, unit).transpose(1, 0, 2)
        pieces = lax.all_to_all(pieces, "z", split_axis=0, concat_axis=0, tiled=True)
        return lax.all_gather(pieces, "xc", axis=1, tiled=False).reshape(width, unit)

    gate_weight, up_weight, down_weight = spread(w_gate), spread(w_up), spread(w_down)
    grad_all = lax.all_gather(cotangent, ("z", "mp"), axis=0, tiled=True)

    query = jnp.dot(normed_one, query_weight, preferred_element_type=jnp.float32).reshape(
        seq_len, heads_here, head_dim
    )
    rotated = (rotate(query, cosine[:, None], sine[:, None]) * scale).astype(jnp.bfloat16)
    keyval = jnp.dot(normed_one, kv_weight, preferred_element_type=jnp.float32)
    keys = rotate(keyval[:, :head_dim], cosine, sine).astype(jnp.bfloat16)
    values = keyval[:, head_dim:].astype(jnp.bfloat16)
    allowed = block_allowed(segments, 0, seq_len)
    scores = jnp.einsum("thd,sd->hts", rotated, keys, preferred_element_type=jnp.float32)
    scores = jnp.where(allowed[None], scores, masked_score)
    row_max = jnp.max(scores, axis=-1, keepdims=True)
    weights = jnp.exp(scores - row_max)
    probs = weights / jnp.sum(weights, axis=-1, keepdims=True)
    probs_low = probs.astype(jnp.bfloat16)
    attn_vals = (
        jnp.einsum("hts,sd->thd", probs_low, values, preferred_element_type=jnp.float32)
        .reshape(seq_len, heads_here * head_dim)
        .astype(jnp.bfloat16)
    )
    mid = inputs_f + lax.psum_scatter(
        matmul_nt(attn_vals, out_weight).astype(jnp.bfloat16),
        "mp",
        scatter_dimension=0,
        tiled=True,
    ).astype(jnp.float32)
    normed_two = norm_gain(mid, gain_two).astype(jnp.bfloat16)
    normed_all = lax.all_gather(normed_two, ("z", "mp"), axis=0, tiled=True)

    mixed_part, normed_part, weight_parts = ffn_pass(
        normed_all, grad_all, gate_weight, up_weight, down_weight
    )
    grad_normed_two = lax.psum_scatter(
        normed_part, ("z", "mp"), scatter_dimension=0, tiled=True
    ).astype(jnp.float32)
    mixed = (
        mid
        + lax.psum_scatter(mixed_part, ("z", "mp"), scatter_dimension=0, tiled=True).astype(
            jnp.float32
        )
    ).astype(jnp.bfloat16)

    def collect(part):
        pieces = part.reshape(z_size, xc_size, rows, unit).transpose(1, 0, 2, 3)
        pieces = pieces.reshape(xc_size * z_size * rows, unit)
        pieces = lax.psum_scatter(pieces, "xc", scatter_dimension=0, tiled=True)
        pieces = pieces.reshape(z_size, rows, unit)
        pieces = lax.all_to_all(pieces, "z", split_axis=0, concat_axis=0, tiled=True)
        return pieces.transpose(1, 0, 2).reshape(rows, z_size * unit).astype(jnp.float32)

    w_gate_grad, w_up_grad, w_down_grad = [collect(part) for part in weight_parts]

    norm_pull_two = jax.vjp(norm_gain, mid, gain_two)[1]
    grad_mid_norm, grad_gain_two = norm_pull_two(grad_normed_two)
    grad_mid = cotangent.astype(jnp.float32) + grad_mid_norm
    grad_mid_all = lax.all_gather(grad_mid.astype(jnp.bfloat16), "mp", axis=0, tiled=True)
    grad_vals = (
        jnp.dot(grad_mid_all, out_weight, preferred_element_type=jnp.float32)
        .astype(jnp.bfloat16)
        .reshape(seq_len, heads_here, head_dim)
    )
    grad_probs = jnp.einsum("thd,sd->hts", grad_vals, values, preferred_element_type=jnp.float32)
    delta = jnp.sum(probs * grad_probs, axis=-1, keepdims=True)
    grad_scores = (probs * (grad_probs - delta)).astype(jnp.bfloat16)
    grad_rot = jnp.einsum("hts,sd->thd", grad_scores, keys, preferred_element_type=jnp.float32)
    key_sum = jnp.einsum("hts,thd->sd", grad_scores, rotated, preferred_element_type=jnp.float32)
    value_sum = jnp.einsum("hts,thd->sd", probs_low, grad_vals, preferred_element_type=jnp.float32)
    grad_query = (
        (unrotate(grad_rot, cosine[:, None], sine[:, None]) * scale)
        .reshape(seq_len, heads_here * head_dim)
        .astype(jnp.bfloat16)
    )
    grad_kv = jnp.concatenate([unrotate(key_sum, cosine, sine), value_sum], axis=1).astype(
        jnp.bfloat16
    )
    grad_normed_one = lax.psum_scatter(
        (matmul_nt(grad_query, query_weight) + matmul_nt(grad_kv, kv_weight)).astype(jnp.bfloat16),
        "mp",
        scatter_dimension=0,
        tiled=True,
    ).astype(jnp.float32)
    norm_pull_one = jax.vjp(norm_gain, inputs_f, gain_one)[1]
    grad_input_norm, grad_gain_one = norm_pull_one(grad_normed_one)
    tokens_grad = (grad_mid + grad_input_norm).astype(jnp.bfloat16)

    w_query_grad = lax.psum_scatter(
        matmul_tn(normed_one, grad_query).astype(jnp.bfloat16), dp, scatter_dimension=0, tiled=True
    ).astype(jnp.float32)
    w_out_grad = lax.psum_scatter(
        matmul_tn(grad_mid_all, attn_vals).astype(jnp.bfloat16), dp, scatter_dimension=0, tiled=True
    ).astype(jnp.float32)
    small = jnp.concatenate(
        [matmul_tn(normed_one, grad_kv), grad_gain_one[:, None], grad_gain_two[:, None]], axis=1
    )
    small = lax.psum_scatter(small, everywhere, scatter_dimension=0, tiled=True)
    kv_grad = small[:, : 2 * head_dim]
    return (
        mixed,
        tokens_grad,
        small[:, 2 * head_dim],
        small[:, 2 * head_dim + 1],
        kv_grad,
        w_query_grad,
        w_out_grad,
        w_gate_grad,
        w_up_grad,
        w_down_grad,
    )


def shards_fast(
    tokens,
    segments,
    positions,
    cotangent,
    attn_gain,
    ffn_gain,
    w_kv,
    w_query,
    w_out,
    w_gate,
    w_up,
    w_down,
):
    seq_len = segments.shape[0]
    cosine, sine = rotary_angles(positions, w_kv.shape[1] // 2)
    table = jnp.stack(
        [
            jnp.concatenate([cosine, cosine], axis=1),
            jnp.concatenate([-sine, sine], axis=1),
        ]
    )
    gain_rows = jnp.pad(
        jnp.stack([attn_gain, ffn_gain]).astype(jnp.float32),
        ((0, 6), (0, 128 - attn_gain.shape[0])),
    )
    segment_rows = jnp.broadcast_to(segments.astype(jnp.float32)[None, :], (8, seq_len))
    (
        normed_one,
        rotated,
        keys,
        values,
        attn_vals,
        mid,
        normed_two,
        gains,
        allowed,
        kv_weight,
        query_weight,
        out_weight,
        ffn_weights,
        grad_all,
    ) = pre_call(
        tokens,
        w_kv,
        gain_rows,
        table,
        segment_rows,
        cotangent,
        w_query,
        w_out,
        (w_gate, w_up, w_down),
    )
    main = ragged_split(w_gate.shape[1], lax.axis_size("z"))[0]
    grad_mid, gain_part, mix_parts, ffn_sums, grad_mid_low = ffn_call(
        gains, normed_two, grad_all, ffn_weights, mid, w_gate.shape[0], main
    )
    mixed, tokens_grad, gain_grads, kv_grad, query_grad, out_grad, ffn_grads = post_call(
        tokens,
        gains,
        gain_part,
        normed_one,
        rotated,
        keys,
        values,
        attn_vals,
        table,
        allowed,
        kv_weight,
        query_weight,
        out_weight,
        mix_parts,
        grad_mid,
        grad_mid_low,
        mid,
        ffn_sums,
        main,
    )
    *ffn_out, query_grad, out_grad, kv_grad, mixed, tokens_grad = layout_call(
        ffn_sums,
        ffn_grads,
        query_grad,
        out_grad,
        kv_grad,
        mixed,
        tokens_grad,
        w_gate.shape[1],
    )
    share = attn_gain.shape[0]
    place = lax.axis_index(("z", "x", "c", "mp")) * share
    gain_grads = gain_grads.reshape(2, gain_grads.size // 2)
    gain_grads = lax.dynamic_slice(gain_grads, (0, place), (2, share))
    return (
        mixed,
        tokens_grad,
        gain_grads[0],
        gain_grads[1],
        kv_grad,
        query_grad,
        out_grad,
        *ffn_out,
    )


def solution(mesh):
    dp_size, mp_size = mesh.shape["dp"], mesh.shape["mp"]
    if dp_size == 4 * FF_SPLIT and mp_size == 2:
        body, dp = shards_fast, ("z", "x", "c")
        sizes = (FF_SPLIT, 2, 2, mp_size)
    else:
        body, dp = shards_general, ("z", "xc")
        sizes = (FF_SPLIT, dp_size // FF_SPLIT, mp_size)
    all_axes = (*dp, "mp")
    fine = jax.sharding.Mesh(mesh.devices.reshape(sizes), all_axes)
    in_specs = (
        P(all_axes, None),
        P(dp),
        P(dp),
        P(all_axes, None),
        P(all_axes),
        P(all_axes),
        P(all_axes, None),
        P(dp, "mp"),
        P(dp, "mp"),
        P(dp, "mp"),
        P(dp, "mp"),
        P(dp, "mp"),
    )
    out_specs = (
        P(all_axes, None),
        P(all_axes, None),
        P(all_axes),
        P(all_axes),
        P(all_axes, None),
        P(dp, "mp"),
        P(dp, "mp"),
        P(dp, "mp"),
        P(dp, "mp"),
        P(dp, "mp"),
    )
    return jax.shard_map(body, mesh=fine, in_specs=in_specs, out_specs=out_specs, check_vma=False)
```

```python
import functools

import jax
import jax.numpy as jnp
from jax import lax
from jax.experimental import pallas as pl
from jax.experimental.pallas import tpu as pltpu
from jax.sharding import PartitionSpec as P

WINDOW = 2048


epsilon = 1e-06
rope_base = 10000.0
masked_score = -1e30
VMEM_BYTES = 66_000_000


def norm_gain(values, gain):
    return values * lax.rsqrt(jnp.mean(values * values, axis=-1, keepdims=True) + epsilon) * gain


def rotary_angles(positions, head_width):
    quarter = head_width // 4
    freqs = rope_base ** (-jnp.arange(quarter).astype(jnp.float32) / quarter)
    phase = positions.astype(jnp.float32)[:, None] * freqs[None, :]
    return (jnp.cos(phase), jnp.sin(phase))


def rotate(values, cosine, sine):
    quarter = cosine.shape[-1]
    first_half = values[..., :quarter]
    second_half = values[..., quarter : 2 * quarter]
    return jnp.concatenate(
        [
            first_half * cosine - second_half * sine,
            second_half * cosine + first_half * sine,
            values[..., 2 * quarter :],
        ],
        axis=-1,
    )


def unrotate(values, cosine, sine):
    quarter = cosine.shape[-1]
    first_half = values[..., :quarter]
    second_half = values[..., quarter : 2 * quarter]
    return jnp.concatenate(
        [
            first_half * cosine + second_half * sine,
            second_half * cosine - first_half * sine,
            values[..., 2 * quarter :],
        ],
        axis=-1,
    )


def gelu_product(gate, up_proj):
    return jax.nn.gelu(gate, approximate=True) * up_proj


def matmul_nt(left, right):
    return lax.dot_general(
        left, right, (((1,), (1,)), ((), ())), preferred_element_type=jnp.float32
    )


def matmul_tn(left, right):
    return lax.dot_general(
        left, right, (((0,), (0,)), ((), ())), preferred_element_type=jnp.float32
    )


def block_allowed(segments, first_row, rows):
    seq_len = segments.shape[0]
    query_rows = first_row + jnp.arange(rows)
    key_rows = jnp.arange(seq_len)
    return (
        (segments[:, None] == segments[None, :])
        & (key_rows[None, :] <= query_rows[:, None])
        & (query_rows[:, None] - key_rows[None, :] < WINDOW)
    )


MESH_ID = pl.DeviceIdType.MESH
GELU_A = 0.7978845608028654
GELU_B = 0.044715
TILE = 256
WIDE = 512


def remote(src, dst, send_sem, recv_sem, where):
    return pltpu.make_async_remote_copy(
        src_ref=src,
        dst_ref=dst,
        send_sem=send_sem,
        recv_sem=recv_sem,
        device_id=where,
        device_id_type=MESH_ID,
    )


def dot_nn(left, right):
    return lax.dot_general(
        left, right, (((1,), (0,)), ((), ())), preferred_element_type=jnp.float32
    )


def gelu_parts(gate):
    square = gate * gate
    bend = jnp.tanh(GELU_A * gate * (1.0 + GELU_B * square))
    half = 0.5 * (1.0 + bend)
    slope = half + 0.5 * gate * (1.0 - bend * bend) * GELU_A * (1.0 + 3.0 * GELU_B * square)
    return gate * half, slope


def add_rows(first, rest, out, count):
    def body(index, carry):
        step = pl.ds(pl.multiple_of(index * 32, 32), 32)
        total = first[step, :].astype(jnp.float32)
        for other in rest:
            total = total + other[step, :].astype(jnp.float32)
        out[step, :] = total.astype(out.dtype)
        return carry

    lax.fori_loop(0, count // 32, body, 0)


def norm_back(values, gain, upstream):
    scale = lax.rsqrt(jnp.mean(values * values, axis=-1, keepdims=True) + epsilon)
    normed = values * scale
    pulled = gain * upstream
    back = scale * (pulled - normed * jnp.mean(normed * pulled, axis=-1, keepdims=True))
    return back, jnp.sum(upstream * normed, axis=0, keepdims=True)


def ffn_kernel(
    z_size,
    main,
    gain_ref,
    own_hbm,
    dy_hbm,
    w_hbm,
    mid_hbm,
    gm_ref,
    gain_part,
    mix_hbm,
    sums_hbm,
    gm_hbm,
    n2,
    dy,
    w3,
    h3,
    n2_t,
    dy_t,
    gn_part,
    mix_buf,
    gn_y,
    gn_z,
    gn_s,
    c_in,
    x_in,
    mid,
    load_sem,
    mix_sem,
    ag_y_send,
    ag_y_recv,
    ag_z_send,
    ag_z_recv,
    rs_y_send,
    rs_y_recv,
    rs_z_send,
    rs_z_recv,
    c_send,
    c_recv,
    x_send,
    x_recv,
    out_sem,
):
    own = own_hbm.shape[0] // 2
    width = own_hbm.shape[1]
    units = w3.shape[2]
    rows = c_in.shape[3]
    span = width // z_size
    me_y, me_z = lax.axis_index("mp"), lax.axis_index("z")
    me_x, me_c = lax.axis_index("x"), lax.axis_index("c")
    mine = pl.ds(pl.multiple_of(me_y * own, own), own)
    theirs = pl.ds(pl.multiple_of((1 - me_y) * own, own), own)
    to_y, to_x, to_c = {"mp": 1 - me_y}, {"x": 1 - me_x}, {"c": 1 - me_c}

    def ahead(step):
        return lax.rem(me_z + step, z_size)

    def to_z(step):
        return {"z": ahead(step)}

    def row_block(z_at, x_at, c_at):
        return pl.ds(pl.multiple_of(((z_at * 2 + x_at) * 2 + c_at) * rows, rows), rows)

    inner = (me_z > 0) & (me_z < z_size - 1)
    outer = (me_z == 0) | (me_z == z_size - 1)

    def w_load(index, columns):
        cols = pl.ds(0, columns)
        return pltpu.make_async_copy(
            w_hbm.at[index, :, cols], w3.at[index, :, cols], load_sem.at[z_size + index]
        )

    def w_loads(act):
        for case, columns in ((inner, units), (outer, main)):

            @pl.when(case)
            def _(columns=columns):
                for index in range(3):
                    act(w_load(index, columns))

    w_loads(lambda copy: copy.start())
    dy_loads = [
        pltpu.make_async_copy(dy_hbm.at[index], dy, load_sem.at[index])
        for index in range(z_size)
    ]
    own_load = pltpu.make_async_copy(own_hbm, n2.at[0], load_sem.at[z_size + 3])
    mid_load = pltpu.make_async_copy(mid_hbm, mid, load_sem.at[z_size + 4])
    for load in (own_load, dy_loads[0], mid_load):
        load.start()

    barrier = pltpu.get_barrier_semaphore()
    peers = [to_y, to_x, to_c] + [to_z(step) for step in range(1, z_size)]
    for where in peers:
        pl.semaphore_signal(barrier, inc=1, device_id=where, device_id_type=MESH_ID)
    pl.semaphore_wait(barrier, len(peers))

    def ag_y(index):
        block = n2.at[index, mine]
        return remote(block, block, ag_y_send.at[index], ag_y_recv.at[index], to_y)

    def ag_y_in(index):
        block = n2.at[index, theirs]
        return remote(block, block, ag_y_send.at[index], ag_y_recv.at[index], to_y)

    def ag_z(index):
        src = own_hbm.at[mine] if index == 0 else n2.at[index, mine]
        return remote(
            src, n2.at[index + 1, mine], ag_z_send.at[index], ag_z_recv.at[index + 1], to_z(1)
        )

    def ag_z_in(index):
        block = n2.at[index, mine]
        return remote(block, block, ag_z_send.at[0], ag_z_recv.at[index], to_z(1))

    left, right = pl.ds(0, width // 2), pl.ds(width // 2, width // 2)

    def ag_last_z():
        return remote(
            n2.at[2, theirs, left],
            n2.at[3, theirs, left],
            ag_y_send.at[0],
            ag_y_recv.at[0],
            to_z(1),
        )

    def ag_last_y():
        block = n2.at[3, mine, right]
        return remote(block, block, ag_y_send.at[3], ag_y_recv.at[3], to_y)

    def ag_last_y_in():
        block = n2.at[3, theirs, right]
        return remote(block, block, ag_y_send.at[3], ag_y_recv.at[3], to_y)

    def forward(index):
        ag_z_in(index).wait_recv()
        ag_z(index).start()
        ag_y(index).start()

    ag_z(0).start()

    mix_copies = []

    def turn(source, target, index):
        def turn_tile(tile, carry):
            at = pl.ds(pl.multiple_of(tile * span, 128), span)
            target[at, pl.ds(index * 2 * own, 2 * own)] = source[:, at].T
            return carry

        lax.fori_loop(0, z_size, turn_tile, 0)

    def chunk(index, between=None):
        if index:
            mix_copies[index - 1].wait()
        dy_loads[index].wait()
        rows_at = pl.ds(index * 2 * own, 2 * own)

        def up_tile(tile, carry):
            cols = pl.ds(pl.multiple_of(tile * TILE, TILE), TILE)
            gate = dot_nn(n2[index], w3[0, :, cols])
            up_proj = dot_nn(n2[index], w3[1, :, cols])
            grad_hidden = dot_nn(dy[...], w3[2, :, cols])
            act, slope = gelu_parts(gate)
            h3[0, rows_at, cols] = (grad_hidden * up_proj * slope).astype(jnp.bfloat16)
            h3[1, rows_at, cols] = (grad_hidden * act).astype(jnp.bfloat16)
            h3[2, rows_at, cols] = (act * up_proj).astype(jnp.bfloat16)
            return carry

        lax.fori_loop(0, units // TILE, up_tile, 0)

        if between:
            between()

        def down_tile(tile, carry):
            at = pl.ds(pl.multiple_of(tile * span, 128), span)
            normed = matmul_nt(w3[0, at, :], h3[0, rows_at, :]) + matmul_nt(
                w3[1, at, :], h3[1, rows_at, :]
            )
            mixed = matmul_nt(w3[2, at, :], h3[2, rows_at, :])
            for half in range(2):
                cols = slice(half * own, (half + 1) * own)
                gn_part[index, half, at, :] = normed[:, cols].astype(jnp.bfloat16)
                mix_buf[half, at, :] = mixed[:, cols].astype(jnp.bfloat16)
            return carry

        lax.fori_loop(0, z_size, down_tile, 0)
        copy = pltpu.make_async_copy(mix_buf, mix_hbm.at[index], mix_sem.at[index])
        copy.start()
        mix_copies.append(copy)
        if index:
            rs_y(index).start()
        turn(n2.at[index], n2_t, index)
        turn(dy, dy_t, index)
        if index + 1 < z_size:
            dy_loads[index + 1].start()

    def rs_y(index):
        return remote(
            gn_part.at[index, 1 - me_y], gn_y.at[index], rs_y_send.at[index], rs_y_recv.at[index], to_y
        )

    def rs_z(index):
        return remote(
            gn_s.at[index - 1],
            gn_z.at[index - 1],
            rs_z_send.at[index],
            rs_z_recv.at[index - 1],
            to_z(1),
        )

    def rs_step(index):
        rs_y(index).wait_recv()
        slot = (index - 2) % z_size
        if index != 1:
            remote(
                gn_s.at[slot], gn_z.at[slot], rs_z_send.at[1], rs_z_recv.at[slot], to_z(1)
            ).wait_recv()

        def add_tile(tile, carry):
            at = pl.ds(pl.multiple_of(tile * TILE, TILE), TILE)
            total = gn_part[index, me_y, at, :].astype(jnp.float32) + gn_y[index, at, :].astype(
                jnp.float32
            )
            if index != 1:
                total = total + gn_z[slot, at, :].astype(jnp.float32)
            if index == 0:
                gm_ref[:, at] = total.T
            else:
                gn_s[index - 1, at, :] = total.astype(jnp.bfloat16)
            return carry

        lax.fori_loop(0, width // TILE, add_tile, 0)
        if index != 0:
            rs_z(index).start()


    def grads(step):
        at = pl.ds(pl.multiple_of(ahead(step) * span, 128), span)
        for kind, source in enumerate((n2_t, n2_t, dy_t)):

            def tile_body(tile, carry, kind=kind, source=source):
                cols = pl.ds(pl.multiple_of(tile * WIDE, WIDE), WIDE)
                w3[kind, at, cols] = dot_nn(source[at, :], h3[kind, :, cols]).astype(jnp.bfloat16)
                return carry

            lax.fori_loop(0, units // WIDE, tile_body, 0)
        for far in (1, 0):
            for kind in range(3):
                over_c(kind, step, far).start()

    def over_c(kind, step, far):
        x_at = 1 - me_x if far else me_x
        return remote(
            w3.at[kind, row_block(ahead(step), x_at, 1 - me_c)],
            c_in.at[kind, step, far],
            c_send.at[kind, step, far],
            c_recv.at[kind, step, far],
            to_c,
        )

    def over_x(kind):
        return remote(
            w3.at[kind, row_block(ahead(1), 1 - me_x, me_c)],
            x_in.at[kind],
            x_send.at[kind],
            x_recv.at[kind],
            to_x,
        )

    out_copies = []

    def keep(kind, step, far, block):
        copy = pltpu.make_async_copy(
            block, sums_hbm.at[kind, step, far], out_sem.at[kind, step, far]
        )
        copy.start()
        out_copies.append(copy)

    def core_sums(step):
        for far in (1, 0):
            for kind in range(3):
                over_c(kind, step, far).wait_recv()
                x_at = 1 - me_x if far else me_x
                block = w3.at[kind, row_block(ahead(step), x_at, me_c)]
                add_rows(block, [c_in.at[kind, step, far]], block, rows)
                if step != 1:
                    keep(kind, step, far, block)
                elif far:
                    over_x(kind).start()

    def first_sums():
        for kind in range(3):
            over_x(kind).wait_recv()
            block = w3.at[kind, row_block(ahead(1), me_x, me_c)]
            add_rows(block, [x_in.at[kind]], block, rows)
            keep(kind, 1, 0, block)

    own_load.wait()
    w_loads(lambda copy: copy.wait())

    @pl.when(outer)
    def _():
        w3[:, :, main:] = jnp.zeros((3, width, units - main), jnp.bfloat16)

    chunk(0)
    forward(1)
    forward(2)
    ag_y_in(1).wait_recv()
    chunk(1)
    ag_y_in(2).wait_recv()
    ag_last_z().start()
    ag_z_in(3).wait_recv()
    ag_last_y().start()
    chunk(2, lambda: rs_step(1))
    ag_last_z().wait_recv()
    ag_last_y_in().wait_recv()
    chunk(3, lambda: rs_step(2))
    rs_y(0).start()
    grads(1)
    grads(2)
    core_sums(1)
    rs_step(3)
    grads(3)
    core_sums(2)
    grads(0)
    core_sums(3)
    rs_step(0)
    core_sums(0)

    cot_load = pltpu.make_async_copy(
        dy_hbm.at[0, mine], dy.at[pl.ds(0, own)], load_sem.at[z_size + 3]
    )
    cot_load.start()
    cot_load.wait()
    mid_load.wait()

    def mid_rows(index, total):
        at = pl.ds(pl.multiple_of(index * 32, 32), 32)
        grad, gain_sum = norm_back(mid[at, :], gain_ref[1:2, :], gm_ref[at, :])
        grad = grad + dy[at, :].astype(jnp.float32)
        gm_ref[at, :] = grad
        dy[pl.ds(pl.multiple_of(own + index * 32, 32), 32), :] = grad.astype(jnp.bfloat16)
        return total + gain_sum

    gain_sum = lax.fori_loop(0, own // 32, mid_rows, jnp.zeros((1, width), jnp.float32))
    gm_save = pltpu.make_async_copy(dy.at[pl.ds(own, own)], gm_hbm, load_sem.at[z_size + 3])
    gm_save.start()
    for index in range(4):
        gain_part[index : index + 1, :] = jnp.zeros((1, span), jnp.float32)
        gain_part[4 + index : 5 + index, :] = gain_sum[:, index * span : (index + 1) * span]
    first_sums()
    gm_save.wait()

    for copy in mix_copies[3:] + out_copies:
        copy.wait()
    for index in range(z_size):
        if index in (1, 2):
            ag_y(index).wait_send()
        if index == 3:
            ag_last_z().wait_send()
            ag_last_y().wait_send()
        rs_y(index).wait_send()
        if index < z_size - 1:
            ag_z(index).wait_send()
        if index:
            rs_z(index).wait_send()
        for kind in range(3):
            over_c(kind, index, 0).wait_send()
            over_c(kind, index, 1).wait_send()
            if index == 1:
                over_x(kind).wait_send()


def ffn_call(gains, normed, grad_all, weights, mid, rows, main):
    z_size = lax.axis_size("z")
    pair, width = normed.shape
    units = weights.shape[2]
    own = pair // 2
    wide = lambda *lead: pltpu.VMEM((*lead, width), jnp.bfloat16)
    tall = lambda *lead: pltpu.VMEM((*lead, width, own), jnp.bfloat16)
    dma = lambda *lead: pltpu.SemaphoreType.DMA(lead)
    vmem = pl.BlockSpec(memory_space=pltpu.VMEM)
    hbm = pl.BlockSpec(memory_space=pl.ANY)
    return pl.pallas_call(
        functools.partial(ffn_kernel, z_size, main),
        out_shape=(
            jax.ShapeDtypeStruct((own, width), jnp.float32),
            jax.ShapeDtypeStruct((8, width // z_size), jnp.float32),
            jax.ShapeDtypeStruct((z_size, 2, width, own), jnp.bfloat16),
            jax.ShapeDtypeStruct((3, z_size, 2, rows, units), jnp.bfloat16),
            jax.ShapeDtypeStruct((own, width), jnp.bfloat16),
        ),
        in_specs=[vmem, hbm, hbm, hbm, hbm],
        out_specs=(vmem, vmem, hbm, hbm, hbm),
        scratch_shapes=[
            wide(z_size, pair),
            wide(pair),
            pltpu.VMEM(weights.shape, jnp.bfloat16),
            pltpu.VMEM((3, z_size * pair, units), jnp.bfloat16),
            pltpu.VMEM((width, z_size * pair), jnp.bfloat16),
            pltpu.VMEM((width, z_size * pair), jnp.bfloat16),
            tall(z_size, 2),
            tall(2),
            tall(z_size),
            tall(z_size - 1),
            tall(z_size - 1),
            pltpu.VMEM((3, z_size, 2, rows, units), jnp.bfloat16),
            pltpu.VMEM((3, rows, units), jnp.bfloat16),
            pltpu.VMEM((own, width), jnp.float32),
            dma(z_size + 5),
            dma(z_size),
            dma(z_size),
            dma(z_size),
            dma(z_size),
            dma(z_size),
            dma(z_size),
            dma(z_size),
            dma(z_size),
            dma(z_size),
            dma(3, z_size, 2),
            dma(3, z_size, 2),
            dma(3),
            dma(3),
            dma(3, z_size, 2),
        ],
        compiler_params=pltpu.CompilerParams(
            collective_id=0, has_side_effects=True, vmem_limit_bytes=VMEM_BYTES
        ),
        cost_estimate=pl.CostEstimate(
            flops=18 * z_size * pair * width * units,
            bytes_accessed=4 * weights.size + 12 * z_size * pair * width,
            transcendentals=z_size * pair * units,
        ),
    )(gains, normed, grad_all, weights, mid)


def spin(values, table):
    first = values[:, : values.shape[1] // 2]
    turned = first * table[0] + pltpu.roll(first, first.shape[1] // 2, 1) * table[1]
    return jnp.concatenate([turned, values[:, values.shape[1] // 2 :]], axis=1)


def spin_back(values, table):
    first = values[:, : values.shape[1] // 2]
    turned = first * table[0] - pltpu.roll(first, first.shape[1] // 2, 1) * table[1]
    return jnp.concatenate([turned, values[:, values.shape[1] // 2 :]], axis=1)


def head_probs(rotated, keys, allowed):
    scores = jnp.where(allowed > 0.5, matmul_nt(rotated, keys), masked_score)
    weights = jnp.exp(scores - jnp.max(scores, axis=-1, keepdims=True))
    return weights / jnp.sum(weights, axis=-1, keepdims=True)


def ragged_split(columns, parts):
    main = columns // parts // 128 * 128
    return main, main + 128


def pre_kernel(
    z_size,
    tok_ref,
    wkv_ref,
    gains_ref,
    table_ref,
    seg_ref,
    cot_hbm,
    wq_hbm,
    wo_hbm,
    wg_hbm,
    wu_hbm,
    wd_hbm,
    n1_ref,
    rot_ref,
    key_ref,
    val_ref,
    att_ref,
    mid_ref,
    n2_ref,
    gain_ref,
    allow_ref,
    kv_out,
    wq_out,
    wo_out,
    w3_out,
    dy_out,
    kv_w,
    q_w,
    o_w,
    tok,
    part,
    part_y,
    query,
    y_send,
    y_recv,
    ky_send,
    ky_recv,
    az_send,
    az_recv,
    ax_send,
    ax_recv,
    ac_send,
    ac_recv,
    fz_send,
    fz_recv,
    fx_send,
    fx_recv,
    fc_send,
    fc_recv,
    dz_send,
    dz_recv,
    dy_send,
    dy_recv,
    local_sem,
):
    me_z, me_x = lax.axis_index("z"), lax.axis_index("x")
    me_c, me_y = lax.axis_index("c"), lax.axis_index("mp")
    own, width = tok_ref.shape
    rows = wq_hbm.shape[0]
    half_rows = wkv_ref.shape[0]
    head = key_ref.shape[1]
    main, units = ragged_split(wg_hbm.shape[1], z_size)
    to_y, to_x, to_c = {"mp": 1 - me_y}, {"x": 1 - me_x}, {"c": 1 - me_c}

    def to_z(step):
        return {"z": lax.rem(me_z + step, z_size)}

    def from_z(step):
        return lax.rem(me_z - step + z_size, z_size)

    def row_block(step, x_at, c_at):
        start = ((from_z(step) * 2 + x_at) * 2 + c_at) * rows
        return pl.ds(pl.multiple_of(start, rows), rows)

    mine = pl.ds(pl.multiple_of(me_y * own, own), own)
    theirs = pl.ds(pl.multiple_of((1 - me_y) * own, own), own)
    bufs = (kv_w, q_w, o_w)
    inputs = (None, wq_hbm, wo_hbm)

    locals_ = []

    def local(src, dst):
        copy = pltpu.make_async_copy(src, dst, local_sem.at[len(locals_)])
        copy.start()
        locals_.append(copy)
        return copy

    here = row_block(0, me_x, me_c)
    own_q = local(wq_hbm, q_w.at[here])
    own_o = local(wo_hbm, o_w.at[here])
    ffn_in = (wg_hbm, wu_hbm, wd_hbm)

    def body_of(target):
        return pl.ds(pl.multiple_of(target * main, 128), main), pl.ds(0, main)

    def tail_of(target):
        start = z_size * main + lax.rem(target + 1, 2) * 128
        return pl.ds(pl.multiple_of(start, 128), 128), pl.ds(main, 128)

    def is_inner(at):
        return (at > 0) & (at < z_size - 1)

    own_f = []
    for kind in range(3):
        src, dst = body_of(me_z)
        own_f.append(local(ffn_in[kind].at[:, src], w3_out.at[kind, here, dst]))

    def own_tail(kind):
        src, dst = tail_of(me_z)
        return pltpu.make_async_copy(
            ffn_in[kind].at[:, src], w3_out.at[kind, here, dst], local_sem.at[12 + kind]
        )

    @pl.when(is_inner(me_z))
    def _():
        for kind in range(3):
            own_tail(kind).start()
    own_d = local(cot_hbm, dy_out.at[0, mine])

    kv_own = pl.ds(pl.multiple_of(here.start + me_y * half_rows, half_rows), half_rows)
    spread = jnp.concatenate([gains_ref[...], jnp.zeros((120, 128), jnp.float32)], axis=0).T
    kv_w[kv_own, : 2 * head] = wkv_ref[...]
    kv_w[kv_own, 2 * head :] = spread[:half_rows, :].astype(jnp.bfloat16)

    barrier = pltpu.get_barrier_semaphore()
    peers = [to_y, to_x, to_c] + [to_z(step) for step in range(1, z_size)]
    for where in peers:
        pl.semaphore_signal(barrier, inc=1, device_id=where, device_id_type=MESH_ID)
    pl.semaphore_wait(barrier, len(peers))

    tok_y = remote(tok_ref, tok.at[mine], y_send.at[1], y_recv.at[1], to_y)
    tok_y_in = remote(tok_ref, tok.at[theirs], y_send.at[1], y_recv.at[1], to_y)
    part_out = remote(part.at[theirs], part_y, y_send.at[2], y_recv.at[2], to_y)
    n2_y = remote(n2_ref.at[mine], n2_ref.at[mine], y_send.at[3], y_recv.at[3], to_y)
    n2_y_in = remote(n2_ref.at[theirs], n2_ref.at[theirs], y_send.at[3], y_recv.at[3], to_y)

    def block_of(kind, step, x_at):
        if kind:
            return row_block(step, x_at, me_c)
        return kv_rows(step, x_at, me_y)

    def kv_rows(step, x_at, y_at):
        start = row_block(step, x_at, me_c).start + y_at * half_rows
        return pl.ds(pl.multiple_of(start, half_rows), half_rows)

    def kv_y(step, far):
        x_at = 1 - me_x if far else me_x
        block = kv_w.at[kv_rows(step, x_at, me_y)]
        slot = step + z_size * far
        return remote(block, block, ky_send.at[slot], ky_recv.at[slot], to_y)

    def kv_y_in(step, far):
        x_at = 1 - me_x if far else me_x
        block = kv_w.at[kv_rows(step, x_at, 1 - me_y)]
        slot = step + z_size * far
        return remote(block, block, ky_send.at[slot], ky_recv.at[slot], to_y)

    def source(kind, step):
        if isinstance(step, int) and step == 0 and kind:
            return inputs[kind]
        return bufs[kind].at[block_of(kind, step, me_x)]

    first_z, last_z = (z_size - 1 - me_z) // (z_size - 1), me_z // (z_size - 1)
    inner = first_z + last_z == 0
    order = (0, 1 + 2 * first_z, 3 - first_z - last_z, 2 - first_z + last_z)
    hops = (
        None,
        (lax.rem(me_z + 1, z_size), 2),
        (lax.rem(me_z + z_size - 1, z_size), 2),
        (lax.rem(3 * (me_z + 3), z_size), lax.rem(2 * me_z + 3, z_size)),
    )

    def a_z_own(kind, right):
        return remote(
            source(kind, 0),
            bufs[kind].at[block_of(kind, 0, me_x)],
            az_send.at[kind, right],
            az_recv.at[kind, 1 if right else z_size - 1],
            to_z(1 if right else z_size - 1),
        )

    def a_z_start(kind):
        @pl.when(last_z == 0)
        def _():
            a_z_own(kind, 1).start()

        @pl.when(first_z == 0)
        def _():
            a_z_own(kind, 0).start()

    def a_z(kind, index):
        target, slot = hops[index]
        block = bufs[kind].at[block_of(kind, order[index], me_x)]
        return remote(
            block, block, az_send.at[kind, 1 + index], az_recv.at[kind, slot], {"z": target}
        )

    def a_z_next(kind, index):
        @pl.when(inner)
        def _():
            a_z(kind, index).start()

    def a_z_done(kind):
        @pl.when(last_z == 0)
        def _():
            a_z_own(kind, 1).wait_send()

        @pl.when(first_z == 0)
        def _():
            a_z_own(kind, 0).wait_send()

        @pl.when(inner)
        def _():
            for index in range(1, z_size):
                a_z(kind, index).wait_send()

    def a_z_in(kind, step):
        block = bufs[kind].at[block_of(kind, step, me_x)]
        return remote(block, block, az_send.at[kind, 0], az_recv.at[kind, step], to_z(1))

    def a_x(kind, step):
        return remote(
            source(kind, step),
            bufs[kind].at[block_of(kind, step, me_x)],
            ax_send.at[kind, step],
            ax_recv.at[kind, step],
            to_x,
        )

    def a_x_in(kind, step):
        block = bufs[kind].at[block_of(kind, step, 1 - me_x)]
        return remote(block, block, ax_send.at[kind, step], ax_recv.at[kind, step], to_x)

    def a_c(kind, step, far):
        x_at = 1 - me_x if far else me_x
        block = bufs[kind].at[row_block(step, x_at, me_c)]
        src = source(kind, step) if kind and not far else block
        slot = step + z_size * far
        return remote(src, block, ac_send.at[kind, slot], ac_recv.at[kind, slot], to_c)

    def a_c_in(kind, step, far):
        x_at = 1 - me_x if far else me_x
        block = bufs[kind].at[row_block(step, x_at, 1 - me_c)]
        slot = step + z_size * far
        return remote(block, block, ac_send.at[kind, slot], ac_recv.at[kind, slot], to_c)

    def f_z(kind, step, act):
        target = lax.rem(me_z + step, z_size)

        def piece(index, src, dst):
            return remote(
                ffn_in[kind].at[:, src],
                w3_out.at[kind, here, dst],
                fz_send.at[kind, step, index],
                fz_recv.at[kind, step, index],
                to_z(step),
            )

        act(piece(0, *body_of(target)))

        @pl.when(is_inner(target))
        def _():
            act(piece(1, *tail_of(target)))

    def f_z_wait(kind, step):
        block = row_block(step, me_x, me_c)

        def piece(index, dst):
            part = w3_out.at[kind, block, dst]
            return remote(
                part, part, fz_send.at[kind, step, index], fz_recv.at[kind, step, index], to_z(step)
            )

        piece(0, pl.ds(0, main)).wait_recv()

        @pl.when(inner)
        def _():
            piece(1, pl.ds(main, 128)).wait_recv()

    def f_x(kind, step, x_at, act):
        for case, columns in ((inner, units), (first_z + last_z > 0, main)):

            @pl.when(case)
            def _(columns=columns):
                block = w3_out.at[kind, row_block(step, x_at, me_c), pl.ds(0, columns)]
                act(remote(block, block, fx_send.at[kind, step], fx_recv.at[kind, step], to_x))

    def f_x_start(kind, step):
        f_x(kind, step, me_x, lambda copy: copy.start())

    def f_x_wait(kind, step):
        f_x(kind, step, 1 - me_x, lambda copy: copy.wait_recv())

    def f_x_done(kind, step):
        f_x(kind, step, me_x, lambda copy: copy.wait_send())

    def f_c(kind, step, far):
        block = w3_out.at[kind, row_block(step, 1 - me_x if far else me_x, me_c)]
        slot = step + z_size * far
        return remote(block, block, fc_send.at[kind, slot], fc_recv.at[kind, slot], to_c)

    def f_c_in(kind, step, far):
        block = w3_out.at[kind, row_block(step, 1 - me_x if far else me_x, 1 - me_c)]
        slot = step + z_size * far
        return remote(block, block, fc_send.at[kind, slot], fc_recv.at[kind, slot], to_c)

    def d_source(step):
        return cot_hbm if isinstance(step, int) else dy_out.at[step, mine]

    def d_z_own(right):
        slot = 1 if right else z_size - 1
        return remote(
            cot_hbm, dy_out.at[slot, mine], dz_send.at[right], dz_recv.at[slot], to_z(slot)
        )

    def d_z_start():
        @pl.when(last_z == 0)
        def _():
            d_z_own(1).start()

        @pl.when(first_z == 0)
        def _():
            d_z_own(0).start()

    def d_z(index):
        target, slot = hops[index]
        return remote(
            dy_out.at[order[index], mine],
            dy_out.at[slot, mine],
            dz_send.at[1 + index],
            dz_recv.at[slot],
            {"z": target},
        )

    def d_z_done():
        @pl.when(last_z == 0)
        def _():
            d_z_own(1).wait_send()

        @pl.when(first_z == 0)
        def _():
            d_z_own(0).wait_send()

        @pl.when(inner)
        def _():
            for index in range(1, z_size):
                d_z(index).wait_send()

    def d_z_in(step):
        block = dy_out.at[step, mine]
        return remote(block, block, dz_send.at[0], dz_recv.at[step], to_z(1))

    def d_y(step):
        return remote(
            d_source(step), dy_out.at[step, mine], dy_send.at[step], dy_recv.at[step], to_y
        )

    def d_y_in(step):
        block = dy_out.at[step, theirs]
        return remote(block, block, dy_send.at[step], dy_recv.at[step], to_y)

    for kind in (1, 0, 2):
        a_z_start(kind)
        a_x(kind, 0).start()
    kv_y(0, 0).start()
    tok_y.start()
    for kind in (1, 2):
        a_c(kind, 0, 0).start()

    for away in (1, 3, 2):
        f_z(0, away, lambda copy: copy.start())
    for at_end, away in ((first_z, 1), (last_z, z_size - 1)):

        @pl.when(at_end > 0)
        def _(away=away):
            for kind in (1, 2):
                f_z(kind, away, lambda copy: copy.start())

    tok[mine, :] = tok_ref[...]
    seq = 2 * own
    query_at = lax.broadcasted_iota(jnp.int32, (seq, seq), 0)
    key_at = lax.broadcasted_iota(jnp.int32, (seq, seq), 1)
    same = seg_ref[...].T[:, :1] == seg_ref[:1, :]
    allowed = same & (key_at <= query_at) & (query_at - key_at < WINDOW)
    allow_ref[...] = jnp.where(allowed, 1.0, 0.0)
    d_y(0).start()

    def from_x(index):
        step = order[index]
        for kind in (1, 0, 2):
            a_x_in(kind, step).wait_recv()
            if kind:
                a_c(kind, step, 1).start()
            else:
                kv_y(step, 1).start()

    def from_y(index):
        step = order[index]
        for far in range(2):
            kv_y_in(step, far).wait_recv()
            a_c(0, step, far).start()

    for index in range(1, z_size):
        step = order[index]
        for kind in (1, 0, 2):
            a_z_in(kind, step).wait_recv()
            a_z_next(kind, index)
            a_x(kind, step).start()
            if kind:
                a_c(kind, step, 0).start()
            else:
                kv_y(step, 0).start()
        if index == z_size - 2:
            d_z_start()
        if index == z_size - 1:
            for copy in own_f:
                copy.wait()

            @pl.when(inner)
            def _():
                for kind in range(3):
                    own_tail(kind).wait()

            for kind in (1, 2):
                for away, sent in ((1, first_z), (3, last_z), (2, 0)):

                    @pl.when(sent == 0 if away != 2 else me_z >= 0)
                    def _(kind=kind, away=away):
                        f_z(kind, away, lambda copy: copy.start())

            for kind in range(3):
                f_x_start(kind, 0)
                f_c(kind, 0, 0).start()
        if index >= 2:
            from_x(index - 2)
            from_y(index - 2)
    for index in (z_size - 2, z_size - 1):
        from_x(index)
        from_y(index)

    def hand_on(kind, step):
        f_z_wait(kind, step)
        f_x_start(kind, step)
        f_c(kind, step, 0).start()

    def cross(kind, step):
        f_x_wait(kind, step)
        f_c(kind, step, 1).start()

    def pass_cotangent(step):
        d_z_in(order[step]).wait_recv()

        @pl.when(inner)
        def _():
            d_z(step).start()

        d_y(order[step]).start()

    def pass_if(case, step):
        @pl.when(case)
        def _():
            pass_cotangent(step)

    outer = first_z + last_z > 0
    tok_y_in.wait_recv()
    own_q.wait()
    own_o.wait()
    for kind in (0, 1):
        for step in range(z_size):
            for far in range(2):
                a_c_in(kind, step, far).wait_recv()

    gains = kv_w[:, 2 * head :].astype(jnp.float32).T[:8, :]
    gain_ref[...] = gains

    def norm_rows(index, carry):
        at = pl.ds(pl.multiple_of(index * 32, 32), 32)
        values = tok[at, :].astype(jnp.float32)
        scale = lax.rsqrt(jnp.mean(values * values, axis=-1, keepdims=True) + epsilon)
        n1_ref[at, :] = (values * scale * gain_ref[0:1, :]).astype(jnp.bfloat16)
        return carry

    lax.fori_loop(0, 2 * own // 32, norm_rows, 0)
    hand_on(0, order[1])
    table = (table_ref[0], table_ref[1])
    key_ref[...] = spin(dot_nn(n1_ref[...], kv_w[:, :head]), table).astype(jnp.bfloat16)
    val_ref[...] = dot_nn(n1_ref[...], kv_w[:, head : 2 * head]).astype(jnp.bfloat16)
    hand_on(0, order[2])
    head_scale = head ** (-0.5)
    heads = att_ref.shape[1] // head

    half_cols = att_ref.shape[1] // 2
    for index in range(2):
        cols = pl.ds(index * half_cols, half_cols)
        query[:, cols] = dot_nn(n1_ref[...], q_w[:, cols])

    def attend(index):
        cols = pl.ds(index * head, head)
        rotated = (spin(query[:, cols], table) * head_scale).astype(jnp.bfloat16)
        rot_ref[:, cols] = rotated
        probs = head_probs(rotated, key_ref[...], allow_ref[...]).astype(jnp.bfloat16)
        att_ref[:, cols] = dot_nn(probs, val_ref[...]).astype(jnp.bfloat16)

    tasks = [
        lambda: (pass_cotangent(1), pass_if(inner, 2)),
        lambda: hand_on(0, order[3]),
        lambda: (cross(0, 0), hand_on(1, order[1])),
        lambda: cross(1, 0),
        lambda: (cross(2, 0), hand_on(1, order[2])),
    ]
    for index in range(heads):
        attend(index)
        if index < len(tasks):
            tasks[index]()
    for step in range(z_size):
        for far in range(2):
            a_c_in(2, step, far).wait_recv()
    saves = [
        local(kv_w, kv_out),
        local(q_w, wq_out),
        local(o_w, wo_out),
    ]
    span = width // 4

    def project(index, carry):
        cols = pl.ds(pl.multiple_of(index * span, span), span)
        part[:, cols] = matmul_nt(att_ref[...], o_w[cols, :]).astype(jnp.bfloat16)
        return carry

    lax.fori_loop(0, 4, project, 0)
    part_out.start()
    hand_on(1, order[3])
    pass_if(outer, 2)
    pass_if(inner, 3)
    cross(0, order[1])
    hand_on(2, order[1])
    part_out.wait_recv()

    def middle(index, carry):
        at = pl.ds(pl.multiple_of(index * 32, 32), 32)
        there = pl.ds(pl.multiple_of(me_y * own + index * 32, 32), 32)
        values = (
            tok_ref[at, :].astype(jnp.float32)
            + part[there, :].astype(jnp.float32)
            + part_y[at, :].astype(jnp.float32)
        )
        mid_ref[at, :] = values
        scale = lax.rsqrt(jnp.mean(values * values, axis=-1, keepdims=True) + epsilon)
        n2_ref[there, :] = (values * scale * gain_ref[1:2, :]).astype(jnp.bfloat16)
        return carry

    lax.fori_loop(0, own // 32, middle, 0)
    n2_y.start()
    hand_on(2, order[2])
    cross(0, order[2])
    cross(0, order[3])
    hand_on(2, order[3])
    pass_if(outer, 3)
    for kind in (1, 2):
        for index in (1, 2, 3):
            cross(kind, order[index])
    for kind in range(3):
        for step in range(z_size):
            for far in range(2):
                f_c_in(kind, step, far).wait_recv()
    for step in range(z_size):
        d_y_in(step).wait_recv()
    n2_y_in.wait_recv()

    for kind in range(3):
        a_z_done(kind)
    d_z_done()
    tok_y.wait_send()
    part_out.wait_send()
    n2_y.wait_send()
    own_d.wait()
    for copy in saves:
        copy.wait()
    for step in range(z_size):
        d_y(step).wait_send()
        for far in range(2):
            kv_y(step, far).wait_send()
        for kind in range(3):
            if step:
                f_z(kind, step, lambda copy: copy.wait_send())
            a_x(kind, step).wait_send()
            f_x_done(kind, step)
            for far in range(2):
                a_c(kind, step, far).wait_send()
                f_c(kind, step, far).wait_send()


def pre_call(tokens, w_kv, gains, table, segments, cotangent, w_query, w_out, ffn):
    z_size = lax.axis_size("z")
    own, width = tokens.shape
    seq = 2 * own
    rows, cols = w_query.shape
    head = table.shape[2] * 2
    units = ragged_split(ffn[0].shape[1], z_size)[1]
    low = lambda *dims: jax.ShapeDtypeStruct(dims, jnp.bfloat16)
    full = lambda *dims: jax.ShapeDtypeStruct(dims, jnp.float32)
    dma = lambda *lead: pltpu.SemaphoreType.DMA(lead)
    vmem = pl.BlockSpec(memory_space=pltpu.VMEM)
    hbm = pl.BlockSpec(memory_space=pl.ANY)
    wide = lambda *lead: pltpu.VMEM((*lead, width), jnp.bfloat16)
    return pl.pallas_call(
        functools.partial(pre_kernel, z_size),
        out_shape=(
            low(seq, width),
            low(seq, cols),
            low(seq, head),
            low(seq, head),
            low(seq, cols),
            full(own, width),
            low(seq, width),
            full(8, width),
            full(seq, seq),
            low(width, 2 * head + 128),
            low(width, cols),
            low(width, cols),
            low(3, width, units),
            low(z_size, seq, width),
        ),
        in_specs=[vmem] * 5 + [hbm] * 6,
        out_specs=(vmem,) * 9 + (hbm,) * 5,
        scratch_shapes=[
            pltpu.VMEM((width, 2 * head + 128), jnp.bfloat16),
            pltpu.VMEM((width, cols), jnp.bfloat16),
            pltpu.VMEM((width, cols), jnp.bfloat16),
            wide(seq),
            wide(seq),
            wide(own),
            pltpu.VMEM((seq, cols), jnp.float32),
            dma(4),
            dma(4),
            dma(2 * z_size),
            dma(2 * z_size),
            dma(3, z_size + 1),
            dma(3, z_size),
            dma(3, z_size),
            dma(3, z_size),
            dma(3, 2 * z_size),
            dma(3, 2 * z_size),
            dma(3, z_size, 2),
            dma(3, z_size, 2),
            dma(3, z_size),
            dma(3, z_size),
            dma(3, 2 * z_size),
            dma(3, 2 * z_size),
            dma(z_size + 1),
            dma(z_size),
            dma(z_size),
            dma(z_size),
            dma(16),
        ],
        compiler_params=pltpu.CompilerParams(
            collective_id=1, has_side_effects=True, vmem_limit_bytes=VMEM_BYTES
        ),
        cost_estimate=pl.CostEstimate(
            flops=8 * seq * width * cols,
            bytes_accessed=8 * width * (cols + units),
            transcendentals=seq * seq * cols // head,
        ),
    )(tokens, w_kv, gains, table, segments, cotangent, w_query, w_out, *ffn)


def post_kernel(
    z_size,
    main,
    tok_ref,
    gain_ref,
    gain_part_ref,
    n1_ref,
    rot_ref,
    key_ref,
    val_ref,
    att_ref,
    table_ref,
    allow_ref,
    kv_hbm,
    wq_hbm,
    wo_hbm,
    mix_hbm,
    gmf_hbm,
    gmb_hbm,
    mid_hbm,
    sums_hbm,
    mixed_ref,
    tgrad_ref,
    gsum_ref,
    kvg_ref,
    qg_ref,
    og_ref,
    ffn_out,
    kv_w,
    q_w,
    o_w,
    o_part,
    gm,
    gm_f,
    gq,
    gkv,
    kv_sum,
    back_y,
    mix_y,
    mix_z,
    mix_s,
    o_c,
    o_x,
    o_z,
    q_c,
    q_x,
    q_z,
    kv_y,
    kv_c,
    kv_x,
    kv_z,
    gain_own,
    gain_in,
    ffn_in,
    ffn_own,
    load_sem,
    own_sem,
    fx_send,
    fx_recv,
    fz_send,
    fz_recv,
    y_send,
    y_recv,
    my_send,
    my_recv,
    mz_send,
    mz_recv,
    wc_send,
    wc_recv,
    wx_send,
    wx_recv,
    wz_send,
    wz_recv,
    kc_send,
    kc_recv,
    kz_send,
    kz_recv,
    g_send,
    g_recv,
):
    me_z, me_x = lax.axis_index("z"), lax.axis_index("x")
    me_c, me_y = lax.axis_index("c"), lax.axis_index("mp")
    own, width = tok_ref.shape
    seq = 2 * own
    head = key_ref.shape[1]
    cols_here = att_ref.shape[1]
    heads = cols_here // head
    rows = qg_ref.shape[0]
    span = width // z_size
    mine = pl.ds(pl.multiple_of(me_y * own, own), own)
    theirs = pl.ds(pl.multiple_of((1 - me_y) * own, own), own)
    to_y, to_x, to_c = {"mp": 1 - me_y}, {"x": 1 - me_x}, {"c": 1 - me_c}
    head_scale = head ** (-0.5)

    def behind(step):
        return lax.rem(me_z - step + z_size, z_size)

    def to_z(step):
        return {"z": lax.rem(me_z + step, z_size)}

    def row_block(step, x_at, c_at):
        start = ((behind(step) * 2 + x_at) * 2 + c_at) * rows
        return pl.ds(pl.multiple_of(start, rows), rows)

    loads = [
        pltpu.make_async_copy(wo_hbm, o_w, load_sem.at[0]),
        pltpu.make_async_copy(wq_hbm, q_w, load_sem.at[1]),
        pltpu.make_async_copy(
            kv_hbm.at[:, :, :, :, :, pl.ds(0, 2 * head)], kv_w, load_sem.at[2]
        ),
    ]
    for step in range(z_size):
        loads.append(
            pltpu.make_async_copy(mix_hbm.at[step, me_y], mix_s.at[step], load_sem.at[3 + step])
        )
    loads.append(pltpu.make_async_copy(gmf_hbm, gm_f, load_sem.at[3 + z_size]))
    loads.append(pltpu.make_async_copy(gmb_hbm, gm.at[mine], load_sem.at[4 + z_size]))
    mid_load = pltpu.make_async_copy(mid_hbm, gm_f, load_sem.at[5 + z_size])
    for load in loads:
        load.start()

    barrier = pltpu.get_barrier_semaphore()
    peers = [to_y, to_x, to_c] + [to_z(step) for step in range(1, z_size)]
    for where in peers:
        pl.semaphore_signal(barrier, inc=1, device_id=where, device_id_type=MESH_ID)
    pl.semaphore_wait(barrier, len(peers))

    tasks = [(step, kind) for step in (2, 3) for kind in range(3)]

    def f_x(index):
        step, kind = tasks[index]
        return remote(
            sums_hbm.at[kind, step, 1],
            ffn_in.at[index],
            fx_send.at[index],
            fx_recv.at[index],
            to_x,
        )

    def f_own(index):
        step, kind = tasks[index]
        return pltpu.make_async_copy(
            sums_hbm.at[kind, step, 0], ffn_own.at[index % 2], own_sem.at[index % 2]
        )

    def f_z(step, kind, source_z, act):
        for case, columns in (
            ((source_z > 0) & (source_z < z_size - 1), ffn_out.shape[3]),
            ((source_z == 0) | (source_z == z_size - 1), main),
        ):

            @pl.when(case)
            def _(columns=columns):
                cols = pl.ds(0, columns)
                if step == 1:
                    src = sums_hbm.at[kind, 1, 0, :, cols]
                else:
                    src = ffn_in.at[tasks.index((step, kind)), :, cols]
                act(
                    remote(
                        src,
                        ffn_out.at[kind, step, :, cols],
                        fz_send.at[kind, step],
                        fz_recv.at[kind, step],
                        to_z(step),
                    )
                )

    def tick(index):
        step, kind = tasks[index]
        f_x(index).wait_recv()
        f_own(index).wait()
        block = ffn_in.at[index]
        add_rows(block, [ffn_own.at[index % 2]], block, rows)
        if index + 2 < len(tasks):
            f_own(index + 2).start()
        f_z(step, kind, me_z, lambda copy: copy.start())

    def f_x_own(kind):
        return remote(
            sums_hbm.at[kind, 0, 1],
            ffn_out.at[kind, 0],
            fx_send.at[len(tasks) + kind],
            fx_recv.at[len(tasks) + kind],
            to_x,
        )

    f_own(0).start()
    f_own(1).start()
    for index in range(len(tasks)):
        f_x(index).start()
    for kind in range(3):
        f_z(1, kind, me_z, lambda copy: copy.start())

    gm_y = remote(gmb_hbm, gm.at[mine], y_send.at[0], y_recv.at[0], to_y)
    gm_y_in = remote(gm.at[theirs], gm.at[theirs], y_send.at[0], y_recv.at[0], to_y)
    gm_y.start()

    first_z, last_z = (z_size - 1 - me_z) // (z_size - 1), me_z // (z_size - 1)
    inner = first_z + last_z == 0
    order = (
        0,
        1 + (me_z + 1) // 2,
        2 + (2 * me_z - 3) * (1 - first_z - last_z),
        3 - 2 * (me_z // 2),
    )
    right = (None, 1 - me_z // 2, (3 - me_z) * (2 - me_z) // 6 + me_z // 2 * (1 - last_z), 1 - me_z // 2)

    def hop_slot(index):
        step, way = order[index], right[index]
        return way * lax.rem(step + 1, z_size) + (1 - way) * (step - 1 + 4 * ((3 - step) // 2))

    def hop_target(index):
        return {"z": me_z + 2 * right[index] - 1}

    def mix_over_y(step):
        return remote(
            mix_hbm.at[step, 1 - me_y], mix_y.at[step], my_send.at[step], my_recv.at[step], to_y
        )

    def mix_over_z(index):
        slot = hop_slot(index)
        return remote(
            mix_s.at[order[index]],
            mix_z.at[slot],
            mz_send.at[index],
            mz_recv.at[slot],
            hop_target(index),
        )

    def mix_z_in(slot):
        return remote(mix_z.at[slot], mix_z.at[slot], mz_send.at[1], mz_recv.at[slot], to_z(1))

    def mix_add(step, others, last):
        def add_tile(tile, carry):
            at = pl.ds(pl.multiple_of(tile * TILE, TILE), TILE)
            total = mix_s[step, at, :].astype(jnp.float32)
            for other in others:
                total = total + other[at, :].astype(jnp.float32)
            if last:
                mixed_ref[:, at] = (gm_f[:, at] + total.T).astype(jnp.bfloat16)
            else:
                mix_s[step, at, :] = total.astype(jnp.bfloat16)
            return carry

        lax.fori_loop(0, width // TILE, add_tile, 0)

    def mix_step(index):
        step = order[index]
        mix_over_y(step).wait_recv()
        from_y = mix_y.at[step]
        if index:

            @pl.when(inner)
            def _():
                mix_z_in(step).wait_recv()
                mix_add(step, [from_y, mix_z.at[step]], False)

            @pl.when(first_z + last_z > 0)
            def _():
                mix_add(step, [from_y], False)

            mix_over_z(index).start()
        else:
            mid_load.wait()

            @pl.when(first_z == 0)
            def _():
                mix_z_in(0).wait_recv()

            @pl.when(last_z == 0)
            def _():
                mix_z_in(z_size).wait_recv()

            @pl.when(inner)
            def _():
                mix_add(0, [from_y, mix_z.at[0], mix_z.at[z_size]], True)

            @pl.when(first_z > 0)
            def _():
                mix_add(0, [from_y, mix_z.at[z_size]], True)

            @pl.when(last_z > 0)
            def _():
                mix_add(0, [from_y, mix_z.at[0]], True)

    for index in (1, 2, 3, 0):
        mix_over_y(order[index]).start()

    kinds = ((o_part, o_c, o_x, o_z, og_ref), (o_w, q_c, q_x, q_z, qg_ref))

    def w_c(kind, step, far):
        x_at = 1 - me_x if far else me_x
        return remote(
            kinds[kind][0].at[row_block(step, x_at, 1 - me_c)],
            kinds[kind][1].at[step, far],
            wc_send.at[kind, step, far],
            wc_recv.at[kind, step, far],
            to_c,
        )

    def w_x(kind, step):
        return remote(
            kinds[kind][0].at[row_block(step, 1 - me_x, me_c)],
            kinds[kind][2].at[step],
            wx_send.at[kind, step],
            wx_recv.at[kind, step],
            to_x,
        )

    def w_z(kind, index):
        step, slot = order[index], hop_slot(index)
        return remote(
            kinds[kind][0].at[row_block(step, me_x, me_c)],
            kinds[kind][3].at[slot],
            wz_send.at[kind, index],
            wz_recv.at[kind, slot],
            hop_target(index),
        )

    def w_z_in(kind, slot):
        block = kinds[kind][3].at[slot]
        return remote(block, block, wz_send.at[kind, 1], wz_recv.at[kind, slot], to_z(1))

    def w_x_stage(kind, index):
        step = order[index]
        w_c(kind, step, 1).wait_recv()
        block = kinds[kind][0].at[row_block(step, 1 - me_x, me_c)]
        add_rows(block, [kinds[kind][1].at[step, 1]], block, rows)
        w_x(kind, step).start()

    def w_z_stage(kind, index):
        part, from_c, from_x, from_z, result = kinds[kind]
        step = order[index]
        w_c(kind, step, 0).wait_recv()
        w_x(kind, step).wait_recv()
        block = part.at[row_block(step, me_x, me_c)]
        others = [from_c.at[step, 0], from_x.at[step]]
        if index:

            @pl.when(inner)
            def _():
                w_z_in(kind, step).wait_recv()
                add_rows(block, [*others, from_z.at[step]], block, rows)

            @pl.when(first_z + last_z > 0)
            def _():
                add_rows(block, others, block, rows)

            w_z(kind, index).start()
        else:

            @pl.when(first_z == 0)
            def _():
                w_z_in(kind, 0).wait_recv()

            @pl.when(last_z == 0)
            def _():
                w_z_in(kind, z_size).wait_recv()

            @pl.when(inner)
            def _():
                add_rows(block, [*others, from_z.at[0], from_z.at[z_size]], result, rows)

            @pl.when(first_z > 0)
            def _():
                add_rows(block, [*others, from_z.at[z_size]], result, rows)

            @pl.when(last_z > 0)
            def _():
                add_rows(block, [*others, from_z.at[0]], result, rows)

    def w_product(kind, index, left, values):
        step = order[index]
        at = pl.ds(pl.multiple_of(behind(step) * span, 128), span)
        turned = left[:, at].T

        def tile_body(tile, carry):
            cols = pl.ds(pl.multiple_of(tile * TILE, TILE), TILE)
            kinds[kind][0][at, cols] = dot_nn(turned, values[:, cols]).astype(jnp.bfloat16)
            return carry

        lax.fori_loop(0, cols_here // TILE, tile_body, 0)
        for far in (1, 0):
            w_c(kind, step, far).start()

    tick(0)
    tick(1)
    loads[-1].wait()
    gm_y_in.wait_recv()
    w_product(0, 1, gm, att_ref)
    w_product(0, 2, gm, att_ref)
    w_x_stage(0, 1)
    w_product(0, 3, gm, att_ref)
    w_x_stage(0, 2)
    tick(2)
    w_product(0, 0, gm, att_ref)
    w_x_stage(0, 3)
    for load in loads[:-1]:
        load.wait()

    kv_sum[...] = jnp.zeros(kv_sum.shape, jnp.float32)
    table = (table_ref[0], table_ref[1])

    for index in range(2):
        cols = pl.ds(index * (cols_here // 2), cols_here // 2)
        gq[:, cols] = dot_nn(gm[...], o_w[:, cols]).astype(jnp.bfloat16)

    def attend_back(index):
        cols = pl.ds(index * head, head)
        grad_vals = gq[:, cols]
        rotated = rot_ref[:, cols]
        probs = head_probs(rotated, key_ref[...], allow_ref[...])
        grad_probs = matmul_nt(grad_vals, val_ref[...])
        delta = jnp.sum(probs * grad_probs, axis=-1, keepdims=True)
        grad_scores = (probs * (grad_probs - delta)).astype(jnp.bfloat16)
        grad_rot = dot_nn(grad_scores, key_ref[...])
        gq[:, cols] = (spin_back(grad_rot, table) * head_scale).astype(jnp.bfloat16)
        kv_sum[0] += matmul_tn(grad_scores, rotated)
        kv_sum[1] += matmul_tn(probs.astype(jnp.bfloat16), grad_vals)

    for index in range(heads):
        attend_back(index)
        if index == 0:
            w_x_stage(0, 0)
        if 3 + index < len(tasks):
            tick(3 + index)
        if index == heads - 1:
            mix_step(1)
    gkv[:, :head] = spin_back(kv_sum[0], table).astype(jnp.bfloat16)
    gkv[:, head:] = kv_sum[1].astype(jnp.bfloat16)

    w_product(1, 1, n1_ref, gq)
    w_product(1, 2, n1_ref, gq)
    w_x_stage(1, 1)
    w_z_stage(0, 1)
    w_product(1, 3, n1_ref, gq)
    w_x_stage(1, 2)
    w_product(1, 0, n1_ref, gq)
    w_x_stage(1, 3)
    w_x_stage(1, 0)
    for kind in range(3):
        f_x_own(kind).start()

    gm_y.wait_send()
    back = gm
    def input_tile(index, carry):
        at = pl.ds(pl.multiple_of(index * span, 128), span)
        back[:, at] = (
            matmul_nt(gq[...], q_w[at, :]) + matmul_nt(gkv[...], kv_w[index].reshape(span, 2 * head))
        ).astype(jnp.bfloat16)
        return carry

    lax.fori_loop(0, z_size, input_tile, 0)
    back_out = remote(back.at[theirs], back_y, y_send.at[1], y_recv.at[1], to_y)
    back_out.start()

    kv_part = kv_w

    def kv_tile(index, carry):
        at = pl.ds(pl.multiple_of(index * span, 128), span)
        product = dot_nn(n1_ref[:, at].T, gkv[...]).astype(jnp.bfloat16)
        kv_part[index] = product.reshape(kv_part.shape[1:])
        return carry

    lax.fori_loop(0, z_size, kv_tile, 0)
    kv_over_y = remote(kv_part.at[:, :, :, 1 - me_y], kv_y, y_send.at[2], y_recv.at[2], to_y)
    kv_over_y.start()
    mix_step(2)
    w_z_stage(0, 2)
    mix_step(3)
    w_z_stage(0, 3)

    back_out.wait_recv()

    def input_rows(index, total):
        at = pl.ds(pl.multiple_of(index * 32, 32), 32)
        there = pl.ds(pl.multiple_of(me_y * own + index * 32, 32), 32)
        upstream = back[there, :].astype(jnp.float32) + back_y[at, :].astype(jnp.float32)
        grad, gain_part = norm_back(
            tok_ref[at, :].astype(jnp.float32), gain_ref[0:1, :], upstream
        )
        tgrad_ref[at, :] = (gm_f[at, :] + grad).astype(jnp.bfloat16)
        return total + gain_part

    attn_gain_part = lax.fori_loop(
        0, own // 32, input_rows, jnp.zeros((1, width), jnp.float32)
    )
    for index in range(4):
        at = slice(index * span, (index + 1) * span)
        gain_own[0, index : index + 1, :] = attn_gain_part[:, at]
        gain_own[0, 4 + index : 5 + index, :] = gain_part_ref[4 + index : 5 + index, :]

    def gain_send(stage, where):
        return remote(
            gain_own.at[stage], gain_in.at[stage], g_send.at[stage], g_recv.at[stage], where
        )

    gain_hops = [gain_send(0, to_y), gain_send(1, to_c), gain_send(2, to_x)]
    gain_last = [
        remote(
            gain_own.at[3], gain_in.at[2 + step], g_send.at[2 + step], g_recv.at[2 + step], to_z(step)
        )
        for step in range(1, z_size)
    ]

    def gain_fold(stage):
        gain_hops[stage].wait_recv()
        gain_own[stage + 1] = gain_own[stage] + gain_in[stage]

    gain_hops[0].start()
    mid_load.start()
    w_z_stage(1, 1)
    w_z_stage(0, 0)
    w_z_stage(1, 2)
    gain_fold(0)
    gain_hops[1].start()
    mix_step(0)
    w_z_stage(1, 3)
    gain_fold(1)
    gain_hops[2].start()
    kv_over_y.wait_recv()

    def kv_add_y(index, carry):
        for x_at in range(2):
            for c_at in range(2):
                block = kv_part.at[index, x_at, c_at, me_y]
                block[...] = (
                    block[...].astype(jnp.float32) + kv_y[index, x_at, c_at].astype(jnp.float32)
                ).astype(jnp.bfloat16)
        return carry

    lax.fori_loop(0, z_size, kv_add_y, 0)
    kv_over_c = remote(
        kv_part.at[:, :, 1 - me_c, me_y], kv_c, kc_send.at[0], kc_recv.at[0], to_c
    )
    kv_over_c.start()
    gain_fold(2)
    for copy in gain_last:
        copy.start()
    kv_over_c.wait_recv()

    def kv_add_c(index, carry):
        for x_at in range(2):
            block = kv_part.at[index, x_at, me_c, me_y]
            block[...] = (
                block[...].astype(jnp.float32) + kv_c[index, x_at].astype(jnp.float32)
            ).astype(jnp.bfloat16)
        return carry

    lax.fori_loop(0, z_size, kv_add_c, 0)
    kv_over_x = remote(
        kv_part.at[:, 1 - me_x, me_c, me_y], kv_x, kc_send.at[1], kc_recv.at[1], to_x
    )
    kv_over_x.start()
    w_z_stage(1, 0)
    kv_over_x.wait_recv()

    def kv_add_x(index, carry):
        block = kv_part.at[index, me_x, me_c, me_y]
        block[...] = (
            block[...].astype(jnp.float32) + kv_x[index].astype(jnp.float32)
        ).astype(jnp.bfloat16)
        return carry

    lax.fori_loop(0, z_size, kv_add_x, 0)
    kv_over_z = [
        remote(
            kv_part.at[lax.rem(me_z + step, z_size), me_x, me_c, me_y],
            kv_z.at[step - 1],
            kz_send.at[step],
            kz_recv.at[step],
            to_z(step),
        )
        for step in range(1, z_size)
    ]
    for copy in kv_over_z:
        copy.start()
    for copy in gain_last:
        copy.wait_recv()
    gsum_ref[...] = gain_own[3] + gain_in[3] + gain_in[4] + gain_in[5]
    for copy in kv_over_z:
        copy.wait_recv()
    kvg_ref[...] = (
        kv_part[me_z, me_x, me_c, me_y].astype(jnp.float32)
        + kv_z[0].astype(jnp.float32)
        + kv_z[1].astype(jnp.float32)
        + kv_z[2].astype(jnp.float32)
    )

    back_out.wait_send()
    kv_over_y.wait_send()
    kv_over_c.wait_send()
    kv_over_x.wait_send()
    for kind in range(3):
        f_x_own(kind).wait()
    for index in range(len(tasks)):
        f_x(index).wait_send()
    for step in range(1, z_size):
        for kind in range(3):
            f_z(step, kind, me_z, lambda copy: copy.wait_send())
            f_z(step, kind, behind(step), lambda copy: copy.wait_recv())
    for copy in gain_hops + gain_last + kv_over_z:
        copy.wait_send()
    for step in range(z_size):
        mix_over_y(step).wait_send()
        if step:
            mix_over_z(step).wait_send()
        for kind in range(2):
            w_c(kind, step, 0).wait_send()
            w_c(kind, step, 1).wait_send()
            w_x(kind, step).wait_send()
            if step:
                w_z(kind, step).wait_send()


def post_call(
    tokens,
    gains,
    gain_part,
    normed_one,
    rotated,
    keys,
    values,
    attn_vals,
    table,
    allowed,
    kv_weight,
    query_weight,
    out_weight,
    mix_parts,
    grad_mid,
    grad_mid_low,
    mid,
    ffn_sums,
    main,
):
    z_size = lax.axis_size("z")
    own, width = tokens.shape
    seq = 2 * own
    head = keys.shape[1]
    cols = attn_vals.shape[1]
    rows = width // (4 * z_size)
    units = ffn_sums.shape[4]
    low = lambda *dims: pltpu.VMEM(dims, jnp.bfloat16)
    full = lambda *dims: pltpu.VMEM(dims, jnp.float32)
    out_full = lambda *dims: jax.ShapeDtypeStruct(dims, jnp.float32)
    out_low = lambda *dims: jax.ShapeDtypeStruct(dims, jnp.bfloat16)
    dma = lambda *lead: pltpu.SemaphoreType.DMA(lead)
    vmem = pl.BlockSpec(memory_space=pltpu.VMEM)
    hbm = pl.BlockSpec(memory_space=pl.ANY)
    z = z_size
    return pl.pallas_call(
        functools.partial(post_kernel, z_size, main),
        out_shape=(
            out_low(own, width),
            out_low(own, width),
            out_full(8, width // z),
            out_full(rows // 2, 2 * head),
            out_full(rows, cols),
            out_full(rows, cols),
            out_low(3, z, rows, units),
        ),
        in_specs=[vmem] * 10 + [hbm] * 8,
        out_specs=(vmem,) * 6 + (hbm,),
        scratch_shapes=[
            low(z, 2, 2, 2, rows // 2, 2 * head),
            low(width, cols),
            low(width, cols),
            low(width, cols),
            low(seq, width),
            full(own, width),
            low(seq, cols),
            low(seq, 2 * head),
            full(2, seq, head),
            low(own, width),
            low(z, width, own),
            low(z + 1, width, own),
            low(z, width, own),
            low(z, 2, rows, cols),
            low(z, rows, cols),
            low(z + 1, rows, cols),
            low(z, 2, rows, cols),
            low(z, rows, cols),
            low(z + 1, rows, cols),
            low(z, 2, 2, rows // 2, 2 * head),
            low(z, 2, rows // 2, 2 * head),
            low(z, rows // 2, 2 * head),
            low(z - 1, rows // 2, 2 * head),
            full(4, 8, width // z),
            full(6, 8, width // z),
            low(6, rows, units),
            low(2, rows, units),
            dma(6 + z),
            dma(2),
            dma(9),
            dma(9),
            dma(3, z),
            dma(3, z),
            dma(3),
            dma(3),
            dma(z),
            dma(z),
            dma(z),
            dma(z + 1),
            dma(2, z, 2),
            dma(2, z, 2),
            dma(2, z),
            dma(2, z),
            dma(2, z),
            dma(2, z + 1),
            dma(2),
            dma(2),
            dma(z),
            dma(z),
            dma(6),
            dma(6),
        ],
        compiler_params=pltpu.CompilerParams(
            collective_id=2, has_side_effects=True, vmem_limit_bytes=VMEM_BYTES
        ),
        cost_estimate=pl.CostEstimate(
            flops=14 * seq * width * cols,
            bytes_accessed=10 * width * cols,
            transcendentals=seq * seq * cols // head,
        ),
    )(
        tokens,
        gains,
        gain_part,
        normed_one,
        rotated,
        keys,
        values,
        attn_vals,
        table,
        allowed,
        kv_weight.reshape(z, 2, 2, 2, rows // 2, kv_weight.shape[1]),
        query_weight,
        out_weight,
        mix_parts,
        grad_mid,
        grad_mid_low,
        mid,
        ffn_sums,
    )


def layout_kernel(
    z_size,
    main,
    sum_ref,
    ffn_ref,
    q_ref,
    o_ref,
    kv_ref,
    mixed_in,
    tgrad_in,
    wg_ref,
    wu_ref,
    wd_ref,
    qg_ref,
    og_ref,
    kvg_ref,
    mixed_ref,
    tgrad_ref,
):
    me_z = lax.axis_index("z")
    for kind, out in enumerate((wg_ref, wu_ref, wd_ref)):
        for step in range(z_size):
            at = lax.rem(me_z - step + z_size, z_size)
            values = ffn_ref[kind, step].astype(jnp.float32)
            if step == 0:
                values = values + sum_ref[kind, 0, 0].astype(jnp.float32)
            body = pl.ds(pl.multiple_of(at * main, 128), main)
            out[:, body] = values[:, :main]

            @pl.when((at > 0) & (at < z_size - 1))
            def _(out=out, at=at, values=values):
                tail = z_size * main + lax.rem(at + 1, 2) * 128
                out[:, pl.ds(pl.multiple_of(tail, 128), 128)] = values[:, main:]
    qg_ref[...] = q_ref[...]
    og_ref[...] = o_ref[...]
    kvg_ref[...] = kv_ref[...]
    mixed_ref[...] = mixed_in[...]
    tgrad_ref[...] = tgrad_in[...]


def layout_call(ffn_sums, ffn_grads, query_grad, out_grad, kv_grad, mixed, tokens_grad, ffn_cols):
    z_size = lax.axis_size("z")
    main, units = ragged_split(ffn_cols, z_size)
    rows, cols = query_grad.shape
    parts = rows // 32
    kv_rows = kv_grad.shape[0] // parts
    full = lambda *dims: jax.ShapeDtypeStruct(dims, jnp.float32)
    row = lambda height, width: pl.BlockSpec((height, width), lambda index: (index, 0))
    own, width = mixed.shape
    share = pl.BlockSpec((own, width // parts), lambda index: (0, index))
    specs = [row(32, cols), row(32, cols), row(kv_rows, kv_grad.shape[1]), share, share]
    return pl.pallas_call(
        functools.partial(layout_kernel, z_size, main),
        grid=(parts,),
        out_shape=(
            *[full(rows, ffn_cols)] * 3,
            full(rows, cols),
            full(rows, cols),
            full(*kv_grad.shape),
            jax.ShapeDtypeStruct(mixed.shape, jnp.bfloat16),
            jax.ShapeDtypeStruct(mixed.shape, jnp.bfloat16),
        ),
        in_specs=[
            pl.BlockSpec((3, 1, 1, 32, units), lambda index: (0, 0, 0, index, 0)),
            pl.BlockSpec((3, z_size, 32, units), lambda index: (0, 0, index, 0)),
            *specs,
        ],
        out_specs=(*[row(32, ffn_cols)] * 3, *specs),
        compiler_params=pltpu.CompilerParams(vmem_limit_bytes=VMEM_BYTES),
    )(ffn_sums, ffn_grads, query_grad, out_grad, kv_grad, mixed, tokens_grad)


FF_SPLIT = 4


def ffn_pass(normed, grad_out, gate_weight, up_weight, down_weight):
    gate = jnp.dot(normed, gate_weight, preferred_element_type=jnp.float32)
    up_proj = jnp.dot(normed, up_weight, preferred_element_type=jnp.float32)
    grad_hidden = jnp.dot(grad_out, down_weight, preferred_element_type=jnp.float32)
    product, pull = jax.vjp(gelu_product, gate, up_proj)
    hidden = product.astype(jnp.bfloat16)
    grad_gate_f, grad_up_f = pull(grad_hidden)
    grad_gate = grad_gate_f.astype(jnp.bfloat16)
    grad_up = grad_up_f.astype(jnp.bfloat16)
    mixed_part = matmul_nt(hidden, down_weight).astype(jnp.bfloat16)
    normed_part = (matmul_nt(grad_gate, gate_weight) + matmul_nt(grad_up, up_weight)).astype(
        jnp.bfloat16
    )
    weight_parts = [
        matmul_tn(normed, grad_gate).astype(jnp.bfloat16),
        matmul_tn(normed, grad_up).astype(jnp.bfloat16),
        matmul_tn(grad_out, hidden).astype(jnp.bfloat16),
    ]
    return mixed_part, normed_part, weight_parts


def shards_general(
    tokens,
    segments,
    positions,
    cotangent,
    attn_gain,
    ffn_gain,
    w_kv,
    w_query,
    w_out,
    w_gate,
    w_up,
    w_down,
):
    everywhere = ("z", "xc", "mp")
    dp = ("z", "xc")
    z_size = lax.axis_size("z")
    xc_size = lax.axis_size("xc")
    gains = lax.all_gather(
        jnp.stack([attn_gain, ffn_gain], axis=1), everywhere, axis=0, tiled=True
    ).astype(jnp.float32)
    gain_one, gain_two = gains[:, 0], gains[:, 1]
    kv_weight = lax.all_gather(w_kv, everywhere, axis=0, tiled=True)
    head_dim = kv_weight.shape[1] // 2
    width = tokens.shape[1]
    seq_len = segments.shape[0]
    heads_here = w_query.shape[1] // head_dim
    scale = head_dim ** (-0.5)
    cosine, sine = rotary_angles(positions, head_dim)
    inputs_f = tokens.astype(jnp.float32)
    tokens_all = lax.all_gather(tokens, "mp", axis=0, tiled=True)
    normed_one = norm_gain(tokens_all.astype(jnp.float32), gain_one).astype(jnp.bfloat16)
    query_weight = lax.all_gather(w_query, dp, axis=0, tiled=True)
    out_weight = lax.all_gather(w_out, dp, axis=0, tiled=True)

    rows = w_gate.shape[0]
    unit = w_gate.shape[1] // z_size

    def spread(weight):
        pieces = weight.reshape(rows, z_size, unit).transpose(1, 0, 2)
        pieces = lax.all_to_all(pieces, "z", split_axis=0, concat_axis=0, tiled=True)
        return lax.all_gather(pieces, "xc", axis=1, tiled=False).reshape(width, unit)

    gate_weight, up_weight, down_weight = spread(w_gate), spread(w_up), spread(w_down)
    grad_all = lax.all_gather(cotangent, ("z", "mp"), axis=0, tiled=True)

    query = jnp.dot(normed_one, query_weight, preferred_element_type=jnp.float32).reshape(
        seq_len, heads_here, head_dim
    )
    rotated = (rotate(query, cosine[:, None], sine[:, None]) * scale).astype(jnp.bfloat16)
    keyval = jnp.dot(normed_one, kv_weight, preferred_element_type=jnp.float32)
    keys = rotate(keyval[:, :head_dim], cosine, sine).astype(jnp.bfloat16)
    values = keyval[:, head_dim:].astype(jnp.bfloat16)
    allowed = block_allowed(segments, 0, seq_len)
    scores = jnp.einsum("thd,sd->hts", rotated, keys, preferred_element_type=jnp.float32)
    scores = jnp.where(allowed[None], scores, masked_score)
    row_max = jnp.max(scores, axis=-1, keepdims=True)
    weights = jnp.exp(scores - row_max)
    probs = weights / jnp.sum(weights, axis=-1, keepdims=True)
    probs_low = probs.astype(jnp.bfloat16)
    attn_vals = (
        jnp.einsum("hts,sd->thd", probs_low, values, preferred_element_type=jnp.float32)
        .reshape(seq_len, heads_here * head_dim)
        .astype(jnp.bfloat16)
    )
    mid = inputs_f + lax.psum_scatter(
        matmul_nt(attn_vals, out_weight).astype(jnp.bfloat16),
        "mp",
        scatter_dimension=0,
        tiled=True,
    ).astype(jnp.float32)
    normed_two = norm_gain(mid, gain_two).astype(jnp.bfloat16)
    normed_all = lax.all_gather(normed_two, ("z", "mp"), axis=0, tiled=True)

    mixed_part, normed_part, weight_parts = ffn_pass(
        normed_all, grad_all, gate_weight, up_weight, down_weight
    )
    grad_normed_two = lax.psum_scatter(
        normed_part, ("z", "mp"), scatter_dimension=0, tiled=True
    ).astype(jnp.float32)
    mixed = (
        mid
        + lax.psum_scatter(mixed_part, ("z", "mp"), scatter_dimension=0, tiled=True).astype(
            jnp.float32
        )
    ).astype(jnp.bfloat16)

    def collect(part):
        pieces = part.reshape(z_size, xc_size, rows, unit).transpose(1, 0, 2, 3)
        pieces = pieces.reshape(xc_size * z_size * rows, unit)
        pieces = lax.psum_scatter(pieces, "xc", scatter_dimension=0, tiled=True)
        pieces = pieces.reshape(z_size, rows, unit)
        pieces = lax.all_to_all(pieces, "z", split_axis=0, concat_axis=0, tiled=True)
        return pieces.transpose(1, 0, 2).reshape(rows, z_size * unit).astype(jnp.float32)

    w_gate_grad, w_up_grad, w_down_grad = [collect(part) for part in weight_parts]

    norm_pull_two = jax.vjp(norm_gain, mid, gain_two)[1]
    grad_mid_norm, grad_gain_two = norm_pull_two(grad_normed_two)
    grad_mid = cotangent.astype(jnp.float32) + grad_mid_norm
    grad_mid_all = lax.all_gather(grad_mid.astype(jnp.bfloat16), "mp", axis=0, tiled=True)
    grad_vals = (
        jnp.dot(grad_mid_all, out_weight, preferred_element_type=jnp.float32)
        .astype(jnp.bfloat16)
        .reshape(seq_len, heads_here, head_dim)
    )
    grad_probs = jnp.einsum("thd,sd->hts", grad_vals, values, preferred_element_type=jnp.float32)
    delta = jnp.sum(probs * grad_probs, axis=-1, keepdims=True)
    grad_scores = (probs * (grad_probs - delta)).astype(jnp.bfloat16)
    grad_rot = jnp.einsum("hts,sd->thd", grad_scores, keys, preferred_element_type=jnp.float32)
    key_sum = jnp.einsum("hts,thd->sd", grad_scores, rotated, preferred_element_type=jnp.float32)
    value_sum = jnp.einsum("hts,thd->sd", probs_low, grad_vals, preferred_element_type=jnp.float32)
    grad_query = (
        (unrotate(grad_rot, cosine[:, None], sine[:, None]) * scale)
        .reshape(seq_len, heads_here * head_dim)
        .astype(jnp.bfloat16)
    )
    grad_kv = jnp.concatenate([unrotate(key_sum, cosine, sine), value_sum], axis=1).astype(
        jnp.bfloat16
    )
    grad_normed_one = lax.psum_scatter(
        (matmul_nt(grad_query, query_weight) + matmul_nt(grad_kv, kv_weight)).astype(jnp.bfloat16),
        "mp",
        scatter_dimension=0,
        tiled=True,
    ).astype(jnp.float32)
    norm_pull_one = jax.vjp(norm_gain, inputs_f, gain_one)[1]
    grad_input_norm, grad_gain_one = norm_pull_one(grad_normed_one)
    tokens_grad = (grad_mid + grad_input_norm).astype(jnp.bfloat16)

    w_query_grad = lax.psum_scatter(
        matmul_tn(normed_one, grad_query).astype(jnp.bfloat16), dp, scatter_dimension=0, tiled=True
    ).astype(jnp.float32)
    w_out_grad = lax.psum_scatter(
        matmul_tn(grad_mid_all, attn_vals).astype(jnp.bfloat16), dp, scatter_dimension=0, tiled=True
    ).astype(jnp.float32)
    small = jnp.concatenate(
        [matmul_tn(normed_one, grad_kv), grad_gain_one[:, None], grad_gain_two[:, None]], axis=1
    )
    small = lax.psum_scatter(small, everywhere, scatter_dimension=0, tiled=True)
    kv_grad = small[:, : 2 * head_dim]
    return (
        mixed,
        tokens_grad,
        small[:, 2 * head_dim],
        small[:, 2 * head_dim + 1],
        kv_grad,
        w_query_grad,
        w_out_grad,
        w_gate_grad,
        w_up_grad,
        w_down_grad,
    )


def shards_fast(
    tokens,
    segments,
    positions,
    cotangent,
    attn_gain,
    ffn_gain,
    w_kv,
    w_query,
    w_out,
    w_gate,
    w_up,
    w_down,
):
    seq_len = segments.shape[0]
    cosine, sine = rotary_angles(positions, w_kv.shape[1] // 2)
    table = jnp.stack(
        [
            jnp.concatenate([cosine, cosine], axis=1),
            jnp.concatenate([-sine, sine], axis=1),
        ]
    )
    gain_rows = jnp.pad(
        jnp.stack([attn_gain, ffn_gain]).astype(jnp.float32),
        ((0, 6), (0, 128 - attn_gain.shape[0])),
    )
    segment_rows = jnp.broadcast_to(segments.astype(jnp.float32)[None, :], (8, seq_len))
    (
        normed_one,
        rotated,
        keys,
        values,
        attn_vals,
        mid,
        normed_two,
        gains,
        allowed,
        kv_weight,
        query_weight,
        out_weight,
        ffn_weights,
        grad_all,
    ) = pre_call(
        tokens,
        w_kv,
        gain_rows,
        table,
        segment_rows,
        cotangent,
        w_query,
        w_out,
        (w_gate, w_up, w_down),
    )
    main = ragged_split(w_gate.shape[1], lax.axis_size("z"))[0]
    grad_mid, gain_part, mix_parts, ffn_sums, grad_mid_low = ffn_call(
        gains, normed_two, grad_all, ffn_weights, mid, w_gate.shape[0], main
    )
    mixed, tokens_grad, gain_grads, kv_grad, query_grad, out_grad, ffn_grads = post_call(
        tokens,
        gains,
        gain_part,
        normed_one,
        rotated,
        keys,
        values,
        attn_vals,
        table,
        allowed,
        kv_weight,
        query_weight,
        out_weight,
        mix_parts,
        grad_mid,
        grad_mid_low,
        mid,
        ffn_sums,
        main,
    )
    *ffn_out, query_grad, out_grad, kv_grad, mixed, tokens_grad = layout_call(
        ffn_sums,
        ffn_grads,
        query_grad,
        out_grad,
        kv_grad,
        mixed,
        tokens_grad,
        w_gate.shape[1],
    )
    share = attn_gain.shape[0]
    place = lax.axis_index(("z", "x", "c", "mp")) * share
    gain_grads = gain_grads.reshape(2, gain_grads.size // 2)
    gain_grads = lax.dynamic_slice(gain_grads, (0, place), (2, share))
    return (
        mixed,
        tokens_grad,
        gain_grads[0],
        gain_grads[1],
        kv_grad,
        query_grad,
        out_grad,
        *ffn_out,
    )


def solution(mesh):
    dp_size, mp_size = mesh.shape["dp"], mesh.shape["mp"]
    if dp_size == 4 * FF_SPLIT and mp_size == 2:
        body, dp = shards_fast, ("z", "x", "c")
        sizes = (FF_SPLIT, 2, 2, mp_size)
    else:
        body, dp = shards_general, ("z", "xc")
        sizes = (FF_SPLIT, dp_size // FF_SPLIT, mp_size)
    all_axes = (*dp, "mp")
    fine = jax.sharding.Mesh(mesh.devices.reshape(sizes), all_axes)
    in_specs = (
        P(all_axes, None),
        P(dp),
        P(dp),
        P(all_axes, None),
        P(all_axes),
        P(all_axes),
        P(all_axes, None),
        P(dp, "mp"),
        P(dp, "mp"),
        P(dp, "mp"),
        P(dp, "mp"),
        P(dp, "mp"),
    )
    out_specs = (
        P(all_axes, None),
        P(all_axes, None),
        P(all_axes),
        P(all_axes),
        P(all_axes, None),
        P(dp, "mp"),
        P(dp, "mp"),
        P(dp, "mp"),
        P(dp, "mp"),
        P(dp, "mp"),
    )
    return jax.shard_map(body, mesh=fine, in_specs=in_specs, out_specs=out_specs, check_vma=False)
```

```python
import functools

import jax
import jax.numpy as jnp
from jax import lax
from jax.experimental import pallas as pl
from jax.experimental.pallas import tpu as pltpu
from jax.sharding import PartitionSpec as P

WINDOW = 2048


epsilon = 1e-06
rope_base = 10000.0
masked_score = -1e30
VMEM_BYTES = 66_000_000


def norm_gain(values, gain):
    return values * lax.rsqrt(jnp.mean(values * values, axis=-1, keepdims=True) + epsilon) * gain


def rotary_angles(positions, head_width):
    quarter = head_width // 4
    freqs = rope_base ** (-jnp.arange(quarter).astype(jnp.float32) / quarter)
    phase = positions.astype(jnp.float32)[:, None] * freqs[None, :]
    return (jnp.cos(phase), jnp.sin(phase))


def rotate(values, cosine, sine):
    quarter = cosine.shape[-1]
    first_half = values[..., :quarter]
    second_half = values[..., quarter : 2 * quarter]
    return jnp.concatenate(
        [
            first_half * cosine - second_half * sine,
            second_half * cosine + first_half * sine,
            values[..., 2 * quarter :],
        ],
        axis=-1,
    )


def unrotate(values, cosine, sine):
    quarter = cosine.shape[-1]
    first_half = values[..., :quarter]
    second_half = values[..., quarter : 2 * quarter]
    return jnp.concatenate(
        [
            first_half * cosine + second_half * sine,
            second_half * cosine - first_half * sine,
            values[..., 2 * quarter :],
        ],
        axis=-1,
    )


def gelu_product(gate, up_proj):
    return jax.nn.gelu(gate, approximate=True) * up_proj


def matmul_nt(left, right):
    return lax.dot_general(
        left, right, (((1,), (1,)), ((), ())), preferred_element_type=jnp.float32
    )


def matmul_tn(left, right):
    return lax.dot_general(
        left, right, (((0,), (0,)), ((), ())), preferred_element_type=jnp.float32
    )


def block_allowed(segments, first_row, rows):
    seq_len = segments.shape[0]
    query_rows = first_row + jnp.arange(rows)
    key_rows = jnp.arange(seq_len)
    return (
        (segments[:, None] == segments[None, :])
        & (key_rows[None, :] <= query_rows[:, None])
        & (query_rows[:, None] - key_rows[None, :] < WINDOW)
    )


MESH_ID = pl.DeviceIdType.MESH
GELU_A = 0.7978845608028654
GELU_B = 0.044715
TILE = 256
WIDE = 512


def remote(src, dst, send_sem, recv_sem, where):
    return pltpu.make_async_remote_copy(
        src_ref=src,
        dst_ref=dst,
        send_sem=send_sem,
        recv_sem=recv_sem,
        device_id=where,
        device_id_type=MESH_ID,
    )


class Halves:
    def __init__(self, src, dst, send_sem, recv_sem, where):
        rows = src.shape[0] // 2
        cuts = [pl.ds(part * rows, rows) for part in range(2)]
        self.copies = [
            remote(src.at[cut], dst.at[cut], send_sem.at[part], recv_sem.at[part], where)
            for part, cut in enumerate(cuts)
        ]

    def start(self):
        for copy in self.copies:
            copy.start()

    def wait_recv(self):
        for copy in self.copies:
            copy.wait_recv()

    def wait_send(self):
        for copy in self.copies:
            copy.wait_send()


def dot_nn(left, right):
    return lax.dot_general(
        left, right, (((1,), (0,)), ((), ())), preferred_element_type=jnp.float32
    )


def gelu_parts(gate):
    square = gate * gate
    bend = jnp.tanh(GELU_A * gate * (1.0 + GELU_B * square))
    half = 0.5 * (1.0 + bend)
    slope = half + 0.5 * gate * (1.0 - bend * bend) * GELU_A * (1.0 + 3.0 * GELU_B * square)
    return gate * half, slope


def add_rows(first, rest, out, count):
    def body(index, carry):
        step = pl.ds(pl.multiple_of(index * 32, 32), 32)
        total = first[step, :].astype(jnp.float32)
        for other in rest:
            total = total + other[step, :].astype(jnp.float32)
        out[step, :] = total.astype(out.dtype)
        return carry

    lax.fori_loop(0, count // 32, body, 0)


def norm_back(values, gain, upstream):
    scale = lax.rsqrt(jnp.mean(values * values, axis=-1, keepdims=True) + epsilon)
    normed = values * scale
    pulled = gain * upstream
    back = scale * (pulled - normed * jnp.mean(normed * pulled, axis=-1, keepdims=True))
    return back, jnp.sum(upstream * normed, axis=0, keepdims=True)


def ffn_kernel(
    z_size,
    main,
    gain_ref,
    own_hbm,
    dy_hbm,
    w_hbm,
    mid_hbm,
    gm_ref,
    gain_part,
    mix_hbm,
    sums_hbm,
    gm_hbm,
    n2,
    dy,
    w3,
    h3,
    n2_t,
    dy_t,
    gn_part,
    mix_buf,
    gn_y,
    gn_z,
    gn_s,
    c_in,
    x_in,
    mid,
    load_sem,
    mix_sem,
    ag_y_send,
    ag_y_recv,
    ag_z_send,
    ag_z_recv,
    rs_y_send,
    rs_y_recv,
    rs_z_send,
    rs_z_recv,
    c_send,
    c_recv,
    x_send,
    x_recv,
    out_sem,
):
    own = own_hbm.shape[0] // 2
    width = own_hbm.shape[1]
    units = w3.shape[2]
    rows = c_in.shape[3]
    span = width // z_size
    me_y, me_z = lax.axis_index("mp"), lax.axis_index("z")
    me_x, me_c = lax.axis_index("x"), lax.axis_index("c")
    mine = pl.ds(pl.multiple_of(me_y * own, own), own)
    theirs = pl.ds(pl.multiple_of((1 - me_y) * own, own), own)
    to_y, to_x, to_c = {"mp": 1 - me_y}, {"x": 1 - me_x}, {"c": 1 - me_c}

    def ahead(step):
        return lax.rem(me_z + step, z_size)

    def to_z(step):
        return {"z": ahead(step)}

    def row_block(z_at, x_at, c_at):
        return pl.ds(pl.multiple_of(((z_at * 2 + x_at) * 2 + c_at) * rows, rows), rows)

    inner = (me_z > 0) & (me_z < z_size - 1)
    outer = (me_z == 0) | (me_z == z_size - 1)

    def w_load(index, columns):
        cols = pl.ds(0, columns)
        return pltpu.make_async_copy(
            w_hbm.at[index, :, cols], w3.at[index, :, cols], load_sem.at[z_size + index]
        )

    def w_loads(act):
        for case, columns in ((inner, units), (outer, main)):

            @pl.when(case)
            def _(columns=columns):
                for index in range(3):
                    act(w_load(index, columns))

    w_loads(lambda copy: copy.start())
    dy_loads = [
        pltpu.make_async_copy(dy_hbm.at[index], dy, load_sem.at[index])
        for index in range(z_size)
    ]
    own_load = pltpu.make_async_copy(own_hbm, n2.at[0], load_sem.at[z_size + 3])
    mid_load = pltpu.make_async_copy(mid_hbm, mid, load_sem.at[z_size + 4])
    for load in (own_load, dy_loads[0], mid_load):
        load.start()

    barrier = pltpu.get_barrier_semaphore()
    peers = [to_y, to_x, to_c] + [to_z(step) for step in range(1, z_size)]
    for where in peers:
        pl.semaphore_signal(barrier, inc=1, device_id=where, device_id_type=MESH_ID)
    pl.semaphore_wait(barrier, len(peers))

    def ag_y(index):
        block = n2.at[index, mine]
        return Halves(block, block, ag_y_send.at[index], ag_y_recv.at[index], to_y)

    def ag_y_in(index):
        block = n2.at[index, theirs]
        return Halves(block, block, ag_y_send.at[index], ag_y_recv.at[index], to_y)

    def ag_z(index):
        src = own_hbm.at[mine] if index == 0 else n2.at[index, mine]
        return Halves(
            src, n2.at[index + 1, mine], ag_z_send.at[index], ag_z_recv.at[index + 1], to_z(1)
        )

    def ag_z_in(index):
        block = n2.at[index, mine]
        return Halves(block, block, ag_z_send.at[0], ag_z_recv.at[index], to_z(1))

    def ag_last():
        return Halves(
            n2.at[2, theirs], n2.at[3, theirs], ag_y_send.at[3], ag_y_recv.at[3], to_z(1)
        )

    def forward(index):
        ag_z_in(index).wait_recv()
        ag_z(index).start()
        ag_y(index).start()

    ag_z(0).start()

    mix_copies = []

    def turn(source, target, index):
        def turn_tile(tile, carry):
            at = pl.ds(pl.multiple_of(tile * span, 128), span)
            target[at, pl.ds(index * 2 * own, 2 * own)] = source[:, at].T
            return carry

        lax.fori_loop(0, z_size, turn_tile, 0)

    def chunk(index):
        if index:
            mix_copies[index - 1].wait()
        dy_loads[index].wait()
        rows_at = pl.ds(index * 2 * own, 2 * own)

        def up_tile(tile, carry):
            cols = pl.ds(pl.multiple_of(tile * TILE, TILE), TILE)
            gate = dot_nn(n2[index], w3[0, :, cols])
            up_proj = dot_nn(n2[index], w3[1, :, cols])
            grad_hidden = dot_nn(dy[...], w3[2, :, cols])
            act, slope = gelu_parts(gate)
            h3[0, rows_at, cols] = (grad_hidden * up_proj * slope).astype(jnp.bfloat16)
            h3[1, rows_at, cols] = (grad_hidden * act).astype(jnp.bfloat16)
            h3[2, rows_at, cols] = (act * up_proj).astype(jnp.bfloat16)
            return carry

        lax.fori_loop(0, units // TILE, up_tile, 0)

        def down_tile(tile, carry):
            at = pl.ds(pl.multiple_of(tile * span, 128), span)
            normed = matmul_nt(w3[0, at, :], h3[0, rows_at, :]) + matmul_nt(
                w3[1, at, :], h3[1, rows_at, :]
            )
            mixed = matmul_nt(w3[2, at, :], h3[2, rows_at, :])
            for half in range(2):
                cols = slice(half * own, (half + 1) * own)
                gn_part[index, half, at, :] = normed[:, cols].astype(jnp.bfloat16)
                mix_buf[half, at, :] = mixed[:, cols].astype(jnp.bfloat16)
            return carry

        lax.fori_loop(0, z_size, down_tile, 0)
        copy = pltpu.make_async_copy(mix_buf, mix_hbm.at[index], mix_sem.at[index])
        copy.start()
        mix_copies.append(copy)
        if index:
            rs_y(index).start()
        turn(n2.at[index], n2_t, index)
        turn(dy, dy_t, index)
        if index + 1 < z_size:
            dy_loads[index + 1].start()

    def rs_y(index):
        return Halves(
            gn_part.at[index, 1 - me_y], gn_y.at[index], rs_y_send.at[index], rs_y_recv.at[index], to_y
        )

    def rs_z(index):
        return Halves(
            gn_s.at[index - 1],
            gn_z.at[index - 1],
            rs_z_send.at[index],
            rs_z_recv.at[index - 1],
            to_z(1),
        )

    def rs_step(index):
        rs_y(index).wait_recv()
        slot = (index - 2) % z_size
        if index != 1:
            Halves(
                gn_s.at[slot], gn_z.at[slot], rs_z_send.at[1], rs_z_recv.at[slot], to_z(1)
            ).wait_recv()

        def add_tile(tile, carry):
            at = pl.ds(pl.multiple_of(tile * TILE, TILE), TILE)
            total = gn_part[index, me_y, at, :].astype(jnp.float32) + gn_y[index, at, :].astype(
                jnp.float32
            )
            if index != 1:
                total = total + gn_z[slot, at, :].astype(jnp.float32)
            if index == 0:
                gm_ref[:, at] = total.T
            else:
                gn_s[index - 1, at, :] = total.astype(jnp.bfloat16)
            return carry

        lax.fori_loop(0, width // TILE, add_tile, 0)
        if index != 0:
            rs_z(index).start()


    def grads(step):
        at = pl.ds(pl.multiple_of(ahead(step) * span, 128), span)
        for kind, source in enumerate((n2_t, n2_t, dy_t)):

            def tile_body(tile, carry, kind=kind, source=source):
                cols = pl.ds(pl.multiple_of(tile * WIDE, WIDE), WIDE)
                w3[kind, at, cols] = dot_nn(source[at, :], h3[kind, :, cols]).astype(jnp.bfloat16)
                return carry

            lax.fori_loop(0, units // WIDE, tile_body, 0)
        for far in (1, 0):
            for kind in range(3):
                over_c(kind, step, far).start()

    def over_c(kind, step, far):
        x_at = 1 - me_x if far else me_x
        return remote(
            w3.at[kind, row_block(ahead(step), x_at, 1 - me_c)],
            c_in.at[kind, step, far],
            c_send.at[kind, step, far],
            c_recv.at[kind, step, far],
            to_c,
        )

    def over_x(kind):
        return remote(
            w3.at[kind, row_block(ahead(1), 1 - me_x, me_c)],
            x_in.at[kind],
            x_send.at[kind],
            x_recv.at[kind],
            to_x,
        )

    out_copies = []

    def keep(kind, step, far, block):
        copy = pltpu.make_async_copy(
            block, sums_hbm.at[kind, step, far], out_sem.at[kind, step, far]
        )
        copy.start()
        out_copies.append(copy)

    def core_sums(step):
        for far in (1, 0):
            for kind in range(3):
                over_c(kind, step, far).wait_recv()
                x_at = 1 - me_x if far else me_x
                block = w3.at[kind, row_block(ahead(step), x_at, me_c)]
                add_rows(block, [c_in.at[kind, step, far]], block, rows)
                if step != 1:
                    keep(kind, step, far, block)
                elif far:
                    over_x(kind).start()

    def first_sums():
        for kind in range(3):
            over_x(kind).wait_recv()
            block = w3.at[kind, row_block(ahead(1), me_x, me_c)]
            add_rows(block, [x_in.at[kind]], block, rows)
            keep(kind, 1, 0, block)

    own_load.wait()
    w_loads(lambda copy: copy.wait())

    @pl.when(outer)
    def _():
        w3[:, :, main:] = jnp.zeros((3, width, units - main), jnp.bfloat16)

    chunk(0)
    forward(1)
    forward(2)
    ag_y_in(1).wait_recv()
    chunk(1)
    ag_y_in(2).wait_recv()
    ag_last().start()
    chunk(2)
    rs_step(1)
    ag_z_in(3).wait_recv()
    ag_last().wait_recv()
    chunk(3)
    rs_y(0).start()
    rs_step(2)
    grads(1)
    grads(2)
    core_sums(1)
    rs_step(3)
    grads(3)
    core_sums(2)
    grads(0)
    core_sums(3)
    rs_step(0)
    core_sums(0)

    cot_load = pltpu.make_async_copy(
        dy_hbm.at[0, mine], dy.at[pl.ds(0, own)], load_sem.at[z_size + 3]
    )
    cot_load.start()
    cot_load.wait()
    mid_load.wait()

    def mid_rows(index, total):
        at = pl.ds(pl.multiple_of(index * 32, 32), 32)
        grad, gain_sum = norm_back(mid[at, :], gain_ref[1:2, :], gm_ref[at, :])
        grad = grad + dy[at, :].astype(jnp.float32)
        gm_ref[at, :] = grad
        dy[pl.ds(pl.multiple_of(own + index * 32, 32), 32), :] = grad.astype(jnp.bfloat16)
        return total + gain_sum

    gain_sum = lax.fori_loop(0, own // 32, mid_rows, jnp.zeros((1, width), jnp.float32))
    gm_save = pltpu.make_async_copy(dy.at[pl.ds(own, own)], gm_hbm, load_sem.at[z_size + 3])
    gm_save.start()
    for index in range(4):
        gain_part[index : index + 1, :] = jnp.zeros((1, span), jnp.float32)
        gain_part[4 + index : 5 + index, :] = gain_sum[:, index * span : (index + 1) * span]
    first_sums()
    gm_save.wait()

    for copy in mix_copies[3:] + out_copies:
        copy.wait()
    for index in range(z_size):
        if index in (1, 2):
            ag_y(index).wait_send()
        if index == 3:
            ag_last().wait_send()
        rs_y(index).wait_send()
        if index < z_size - 1:
            ag_z(index).wait_send()
        if index:
            rs_z(index).wait_send()
        for kind in range(3):
            over_c(kind, index, 0).wait_send()
            over_c(kind, index, 1).wait_send()
            if index == 1:
                over_x(kind).wait_send()


def ffn_call(gains, normed, grad_all, weights, mid, rows, main):
    z_size = lax.axis_size("z")
    pair, width = normed.shape
    units = weights.shape[2]
    own = pair // 2
    wide = lambda *lead: pltpu.VMEM((*lead, width), jnp.bfloat16)
    tall = lambda *lead: pltpu.VMEM((*lead, width, own), jnp.bfloat16)
    dma = lambda *lead: pltpu.SemaphoreType.DMA(lead)
    vmem = pl.BlockSpec(memory_space=pltpu.VMEM)
    hbm = pl.BlockSpec(memory_space=pl.ANY)
    return pl.pallas_call(
        functools.partial(ffn_kernel, z_size, main),
        out_shape=(
            jax.ShapeDtypeStruct((own, width), jnp.float32),
            jax.ShapeDtypeStruct((8, width // z_size), jnp.float32),
            jax.ShapeDtypeStruct((z_size, 2, width, own), jnp.bfloat16),
            jax.ShapeDtypeStruct((3, z_size, 2, rows, units), jnp.bfloat16),
            jax.ShapeDtypeStruct((own, width), jnp.bfloat16),
        ),
        in_specs=[vmem, hbm, hbm, hbm, hbm],
        out_specs=(vmem, vmem, hbm, hbm, hbm),
        scratch_shapes=[
            wide(z_size, pair),
            wide(pair),
            pltpu.VMEM(weights.shape, jnp.bfloat16),
            pltpu.VMEM((3, z_size * pair, units), jnp.bfloat16),
            pltpu.VMEM((width, z_size * pair), jnp.bfloat16),
            pltpu.VMEM((width, z_size * pair), jnp.bfloat16),
            tall(z_size, 2),
            tall(2),
            tall(z_size),
            tall(z_size - 1),
            tall(z_size - 1),
            pltpu.VMEM((3, z_size, 2, rows, units), jnp.bfloat16),
            pltpu.VMEM((3, rows, units), jnp.bfloat16),
            pltpu.VMEM((own, width), jnp.float32),
            dma(z_size + 5),
            dma(z_size),
            dma(z_size, 2),
            dma(z_size, 2),
            dma(z_size, 2),
            dma(z_size, 2),
            dma(z_size, 2),
            dma(z_size, 2),
            dma(z_size, 2),
            dma(z_size, 2),
            dma(3, z_size, 2),
            dma(3, z_size, 2),
            dma(3),
            dma(3),
            dma(3, z_size, 2),
        ],
        compiler_params=pltpu.CompilerParams(
            collective_id=0, has_side_effects=True, vmem_limit_bytes=VMEM_BYTES
        ),
        cost_estimate=pl.CostEstimate(
            flops=18 * z_size * pair * width * units,
            bytes_accessed=4 * weights.size + 12 * z_size * pair * width,
            transcendentals=z_size * pair * units,
        ),
    )(gains, normed, grad_all, weights, mid)


def spin(values, table):
    first = values[:, : values.shape[1] // 2]
    turned = first * table[0] + pltpu.roll(first, first.shape[1] // 2, 1) * table[1]
    return jnp.concatenate([turned, values[:, values.shape[1] // 2 :]], axis=1)


def spin_back(values, table):
    first = values[:, : values.shape[1] // 2]
    turned = first * table[0] - pltpu.roll(first, first.shape[1] // 2, 1) * table[1]
    return jnp.concatenate([turned, values[:, values.shape[1] // 2 :]], axis=1)


def head_probs(rotated, keys, allowed):
    scores = jnp.where(allowed > 0.5, matmul_nt(rotated, keys), masked_score)
    weights = jnp.exp(scores - jnp.max(scores, axis=-1, keepdims=True))
    return weights / jnp.sum(weights, axis=-1, keepdims=True)


def ragged_split(columns, parts):
    main = columns // parts // 128 * 128
    return main, main + 128


def pre_kernel(
    z_size,
    tok_ref,
    wkv_ref,
    gains_ref,
    table_ref,
    seg_ref,
    cot_hbm,
    wq_hbm,
    wo_hbm,
    wg_hbm,
    wu_hbm,
    wd_hbm,
    n1_ref,
    rot_ref,
    key_ref,
    val_ref,
    att_ref,
    mid_ref,
    n2_ref,
    gain_ref,
    allow_ref,
    kv_out,
    wq_out,
    wo_out,
    w3_out,
    dy_out,
    kv_w,
    q_w,
    o_w,
    tok,
    part,
    part_y,
    query,
    y_send,
    y_recv,
    ky_send,
    ky_recv,
    az_send,
    az_recv,
    ax_send,
    ax_recv,
    ac_send,
    ac_recv,
    fz_send,
    fz_recv,
    fx_send,
    fx_recv,
    fc_send,
    fc_recv,
    dz_send,
    dz_recv,
    dy_send,
    dy_recv,
    local_sem,
):
    me_z, me_x = lax.axis_index("z"), lax.axis_index("x")
    me_c, me_y = lax.axis_index("c"), lax.axis_index("mp")
    own, width = tok_ref.shape
    rows = wq_hbm.shape[0]
    half_rows = wkv_ref.shape[0]
    head = key_ref.shape[1]
    main, units = ragged_split(wg_hbm.shape[1], z_size)
    to_y, to_x, to_c = {"mp": 1 - me_y}, {"x": 1 - me_x}, {"c": 1 - me_c}

    def to_z(step):
        return {"z": lax.rem(me_z + step, z_size)}

    def from_z(step):
        return lax.rem(me_z - step + z_size, z_size)

    def row_block(step, x_at, c_at):
        start = ((from_z(step) * 2 + x_at) * 2 + c_at) * rows
        return pl.ds(pl.multiple_of(start, rows), rows)

    mine = pl.ds(pl.multiple_of(me_y * own, own), own)
    theirs = pl.ds(pl.multiple_of((1 - me_y) * own, own), own)
    bufs = (kv_w, q_w, o_w)
    inputs = (None, wq_hbm, wo_hbm)

    locals_ = []

    def local(src, dst):
        copy = pltpu.make_async_copy(src, dst, local_sem.at[len(locals_)])
        copy.start()
        locals_.append(copy)
        return copy

    here = row_block(0, me_x, me_c)
    own_q = local(wq_hbm, q_w.at[here])
    own_o = local(wo_hbm, o_w.at[here])
    ffn_in = (wg_hbm, wu_hbm, wd_hbm)

    def body_of(target):
        return pl.ds(pl.multiple_of(target * main, 128), main), pl.ds(0, main)

    def tail_of(target):
        start = z_size * main + lax.rem(target + 1, 2) * 128
        return pl.ds(pl.multiple_of(start, 128), 128), pl.ds(main, 128)

    def is_inner(at):
        return (at > 0) & (at < z_size - 1)

    own_f = []
    for kind in range(3):
        src, dst = body_of(me_z)
        own_f.append(local(ffn_in[kind].at[:, src], w3_out.at[kind, here, dst]))

    def own_tail(kind):
        src, dst = tail_of(me_z)
        return pltpu.make_async_copy(
            ffn_in[kind].at[:, src], w3_out.at[kind, here, dst], local_sem.at[12 + kind]
        )

    @pl.when(is_inner(me_z))
    def _():
        for kind in range(3):
            own_tail(kind).start()
    own_d = local(cot_hbm, dy_out.at[0, mine])

    kv_own = pl.ds(pl.multiple_of(here.start + me_y * half_rows, half_rows), half_rows)
    spread = jnp.concatenate([gains_ref[...], jnp.zeros((120, 128), jnp.float32)], axis=0).T
    kv_w[kv_own, : 2 * head] = wkv_ref[...]
    kv_w[kv_own, 2 * head :] = spread[:half_rows, :].astype(jnp.bfloat16)

    barrier = pltpu.get_barrier_semaphore()
    peers = [to_y, to_x, to_c] + [to_z(step) for step in range(1, z_size)]
    for where in peers:
        pl.semaphore_signal(barrier, inc=1, device_id=where, device_id_type=MESH_ID)
    pl.semaphore_wait(barrier, len(peers))

    tok_y = remote(tok_ref, tok.at[mine], y_send.at[1], y_recv.at[1], to_y)
    tok_y_in = remote(tok_ref, tok.at[theirs], y_send.at[1], y_recv.at[1], to_y)
    part_out = remote(part.at[theirs], part_y, y_send.at[2], y_recv.at[2], to_y)
    n2_y = remote(n2_ref.at[mine], n2_ref.at[mine], y_send.at[3], y_recv.at[3], to_y)
    n2_y_in = remote(n2_ref.at[theirs], n2_ref.at[theirs], y_send.at[3], y_recv.at[3], to_y)

    def block_of(kind, step, x_at):
        if kind:
            return row_block(step, x_at, me_c)
        return kv_rows(step, x_at, me_y)

    def kv_rows(step, x_at, y_at):
        start = row_block(step, x_at, me_c).start + y_at * half_rows
        return pl.ds(pl.multiple_of(start, half_rows), half_rows)

    def kv_y(step, far):
        x_at = 1 - me_x if far else me_x
        block = kv_w.at[kv_rows(step, x_at, me_y)]
        slot = step + z_size * far
        return remote(block, block, ky_send.at[slot], ky_recv.at[slot], to_y)

    def kv_y_in(step, far):
        x_at = 1 - me_x if far else me_x
        block = kv_w.at[kv_rows(step, x_at, 1 - me_y)]
        slot = step + z_size * far
        return remote(block, block, ky_send.at[slot], ky_recv.at[slot], to_y)

    def source(kind, step):
        if isinstance(step, int) and step == 0 and kind:
            return inputs[kind]
        return bufs[kind].at[block_of(kind, step, me_x)]

    first_z, last_z = (z_size - 1 - me_z) // (z_size - 1), me_z // (z_size - 1)
    inner = first_z + last_z == 0
    order = (0, 1 + 2 * first_z, 3 - first_z - last_z, 2 - first_z + last_z)
    hops = (
        None,
        (lax.rem(me_z + 1, z_size), 2),
        (lax.rem(me_z + z_size - 1, z_size), 2),
        (lax.rem(3 * (me_z + 3), z_size), lax.rem(2 * me_z + 3, z_size)),
    )

    def a_z_own(kind, right):
        return remote(
            source(kind, 0),
            bufs[kind].at[block_of(kind, 0, me_x)],
            az_send.at[kind, right],
            az_recv.at[kind, 1 if right else z_size - 1],
            to_z(1 if right else z_size - 1),
        )

    def a_z_start(kind):
        @pl.when(last_z == 0)
        def _():
            a_z_own(kind, 1).start()

        @pl.when(first_z == 0)
        def _():
            a_z_own(kind, 0).start()

    def a_z(kind, index):
        target, slot = hops[index]
        block = bufs[kind].at[block_of(kind, order[index], me_x)]
        return remote(
            block, block, az_send.at[kind, 1 + index], az_recv.at[kind, slot], {"z": target}
        )

    def a_z_next(kind, index):
        @pl.when(inner)
        def _():
            a_z(kind, index).start()

    def a_z_done(kind):
        @pl.when(last_z == 0)
        def _():
            a_z_own(kind, 1).wait_send()

        @pl.when(first_z == 0)
        def _():
            a_z_own(kind, 0).wait_send()

        @pl.when(inner)
        def _():
            for index in range(1, z_size):
                a_z(kind, index).wait_send()

    def a_z_in(kind, step):
        block = bufs[kind].at[block_of(kind, step, me_x)]
        return remote(block, block, az_send.at[kind, 0], az_recv.at[kind, step], to_z(1))

    def a_x(kind, step):
        return remote(
            source(kind, step),
            bufs[kind].at[block_of(kind, step, me_x)],
            ax_send.at[kind, step],
            ax_recv.at[kind, step],
            to_x,
        )

    def a_x_in(kind, step):
        block = bufs[kind].at[block_of(kind, step, 1 - me_x)]
        return remote(block, block, ax_send.at[kind, step], ax_recv.at[kind, step], to_x)

    def a_c(kind, step, far):
        x_at = 1 - me_x if far else me_x
        block = bufs[kind].at[row_block(step, x_at, me_c)]
        src = source(kind, step) if kind and not far else block
        slot = step + z_size * far
        return remote(src, block, ac_send.at[kind, slot], ac_recv.at[kind, slot], to_c)

    def a_c_in(kind, step, far):
        x_at = 1 - me_x if far else me_x
        block = bufs[kind].at[row_block(step, x_at, 1 - me_c)]
        slot = step + z_size * far
        return remote(block, block, ac_send.at[kind, slot], ac_recv.at[kind, slot], to_c)

    def f_z(kind, step, act):
        target = lax.rem(me_z + step, z_size)

        def piece(index, src, dst):
            return remote(
                ffn_in[kind].at[:, src],
                w3_out.at[kind, here, dst],
                fz_send.at[kind, step, index],
                fz_recv.at[kind, step, index],
                to_z(step),
            )

        act(piece(0, *body_of(target)))

        @pl.when(is_inner(target))
        def _():
            act(piece(1, *tail_of(target)))

    def f_z_wait(kind, step):
        block = row_block(step, me_x, me_c)

        def piece(index, dst):
            part = w3_out.at[kind, block, dst]
            return remote(
                part, part, fz_send.at[kind, step, index], fz_recv.at[kind, step, index], to_z(step)
            )

        piece(0, pl.ds(0, main)).wait_recv()

        @pl.when(inner)
        def _():
            piece(1, pl.ds(main, 128)).wait_recv()

    def f_x(kind, step, x_at, act):
        for case, columns in ((inner, units), (first_z + last_z > 0, main)):

            @pl.when(case)
            def _(columns=columns):
                block = w3_out.at[kind, row_block(step, x_at, me_c), pl.ds(0, columns)]
                act(remote(block, block, fx_send.at[kind, step], fx_recv.at[kind, step], to_x))

    def f_x_start(kind, step):
        f_x(kind, step, me_x, lambda copy: copy.start())

    def f_x_wait(kind, step):
        f_x(kind, step, 1 - me_x, lambda copy: copy.wait_recv())

    def f_x_done(kind, step):
        f_x(kind, step, me_x, lambda copy: copy.wait_send())

    def f_c(kind, step, far):
        block = w3_out.at[kind, row_block(step, 1 - me_x if far else me_x, me_c)]
        slot = step + z_size * far
        return remote(block, block, fc_send.at[kind, slot], fc_recv.at[kind, slot], to_c)

    def f_c_in(kind, step, far):
        block = w3_out.at[kind, row_block(step, 1 - me_x if far else me_x, 1 - me_c)]
        slot = step + z_size * far
        return remote(block, block, fc_send.at[kind, slot], fc_recv.at[kind, slot], to_c)

    def d_source(step):
        return cot_hbm if isinstance(step, int) else dy_out.at[step, mine]

    def d_z_own(right):
        slot = 1 if right else z_size - 1
        return remote(
            cot_hbm, dy_out.at[slot, mine], dz_send.at[right], dz_recv.at[slot], to_z(slot)
        )

    def d_z_start():
        @pl.when(last_z == 0)
        def _():
            d_z_own(1).start()

        @pl.when(first_z == 0)
        def _():
            d_z_own(0).start()

    def d_z(index):
        target, slot = hops[index]
        return remote(
            dy_out.at[order[index], mine],
            dy_out.at[slot, mine],
            dz_send.at[1 + index],
            dz_recv.at[slot],
            {"z": target},
        )

    def d_z_done():
        @pl.when(last_z == 0)
        def _():
            d_z_own(1).wait_send()

        @pl.when(first_z == 0)
        def _():
            d_z_own(0).wait_send()

        @pl.when(inner)
        def _():
            for index in range(1, z_size):
                d_z(index).wait_send()

    def d_z_in(step):
        block = dy_out.at[step, mine]
        return remote(block, block, dz_send.at[0], dz_recv.at[step], to_z(1))

    def d_y(step):
        return remote(
            d_source(step), dy_out.at[step, mine], dy_send.at[step], dy_recv.at[step], to_y
        )

    def d_y_in(step):
        block = dy_out.at[step, theirs]
        return remote(block, block, dy_send.at[step], dy_recv.at[step], to_y)

    for kind in (1, 0, 2):
        a_z_start(kind)
        a_x(kind, 0).start()
    kv_y(0, 0).start()
    tok_y.start()
    for kind in (1, 2):
        a_c(kind, 0, 0).start()

    for at_end, away in ((first_z, 1), (last_z, z_size - 1)):

        @pl.when(at_end > 0)
        def _(away=away):
            for kind in range(3):
                f_z(kind, away, lambda copy: copy.start())

    tok[mine, :] = tok_ref[...]
    seq = 2 * own
    query_at = lax.broadcasted_iota(jnp.int32, (seq, seq), 0)
    key_at = lax.broadcasted_iota(jnp.int32, (seq, seq), 1)
    same = seg_ref[...].T[:, :1] == seg_ref[:1, :]
    allowed = same & (key_at <= query_at) & (query_at - key_at < WINDOW)
    allow_ref[...] = jnp.where(allowed, 1.0, 0.0)
    d_y(0).start()

    def from_x(index):
        step = order[index]
        for kind in (1, 0, 2):
            a_x_in(kind, step).wait_recv()
            if kind:
                a_c(kind, step, 1).start()
            else:
                kv_y(step, 1).start()

    def from_y(index):
        step = order[index]
        for far in range(2):
            kv_y_in(step, far).wait_recv()
            a_c(0, step, far).start()

    for index in range(1, z_size):
        step = order[index]
        for kind in (1, 0, 2):
            a_z_in(kind, step).wait_recv()
            a_z_next(kind, index)
            a_x(kind, step).start()
            if kind:
                a_c(kind, step, 0).start()
            else:
                kv_y(step, 0).start()
        if index == z_size - 2:
            d_z_start()
        if index == z_size - 1:
            for copy in own_f:
                copy.wait()

            @pl.when(inner)
            def _():
                for kind in range(3):
                    own_tail(kind).wait()

            for kind in range(3):
                for away, sent in ((1, first_z), (3, last_z), (2, 0)):

                    @pl.when(sent == 0 if away != 2 else me_z >= 0)
                    def _(kind=kind, away=away):
                        f_z(kind, away, lambda copy: copy.start())

            for kind in range(3):
                f_x_start(kind, 0)
                f_c(kind, 0, 0).start()
        if index >= 2:
            from_x(index - 2)
            from_y(index - 2)
    for index in (z_size - 2, z_size - 1):
        from_x(index)
        from_y(index)

    def hand_on(kind, step):
        f_z_wait(kind, step)
        f_x_start(kind, step)
        f_c(kind, step, 0).start()

    def cross(kind, step):
        f_x_wait(kind, step)
        f_c(kind, step, 1).start()

    def pass_cotangent(step):
        d_z_in(order[step]).wait_recv()

        @pl.when(inner)
        def _():
            d_z(step).start()

        d_y(order[step]).start()

    def pass_if(case, step):
        @pl.when(case)
        def _():
            pass_cotangent(step)

    outer = first_z + last_z > 0
    tok_y_in.wait_recv()
    own_q.wait()
    own_o.wait()
    for kind in (0, 1):
        for step in range(z_size):
            for far in range(2):
                a_c_in(kind, step, far).wait_recv()

    gains = kv_w[:, 2 * head :].astype(jnp.float32).T[:8, :]
    gain_ref[...] = gains

    def norm_rows(index, carry):
        at = pl.ds(pl.multiple_of(index * 32, 32), 32)
        values = tok[at, :].astype(jnp.float32)
        scale = lax.rsqrt(jnp.mean(values * values, axis=-1, keepdims=True) + epsilon)
        n1_ref[at, :] = (values * scale * gain_ref[0:1, :]).astype(jnp.bfloat16)
        return carry

    lax.fori_loop(0, 2 * own // 32, norm_rows, 0)
    hand_on(0, order[1])
    table = (table_ref[0], table_ref[1])
    key_ref[...] = spin(dot_nn(n1_ref[...], kv_w[:, :head]), table).astype(jnp.bfloat16)
    val_ref[...] = dot_nn(n1_ref[...], kv_w[:, head : 2 * head]).astype(jnp.bfloat16)
    hand_on(0, order[2])
    head_scale = head ** (-0.5)
    heads = att_ref.shape[1] // head

    half_cols = att_ref.shape[1] // 2
    for index in range(2):
        cols = pl.ds(index * half_cols, half_cols)
        query[:, cols] = dot_nn(n1_ref[...], q_w[:, cols])

    def attend(index):
        cols = pl.ds(index * head, head)
        rotated = (spin(query[:, cols], table) * head_scale).astype(jnp.bfloat16)
        rot_ref[:, cols] = rotated
        probs = head_probs(rotated, key_ref[...], allow_ref[...]).astype(jnp.bfloat16)
        att_ref[:, cols] = dot_nn(probs, val_ref[...]).astype(jnp.bfloat16)

    tasks = [
        lambda: (pass_cotangent(1), pass_if(inner, 2)),
        lambda: hand_on(0, order[3]),
        lambda: (cross(0, 0), hand_on(1, order[1])),
        lambda: cross(1, 0),
        lambda: (cross(2, 0), hand_on(1, order[2])),
    ]
    for index in range(heads):
        attend(index)
        if index < len(tasks):
            tasks[index]()
    for step in range(z_size):
        for far in range(2):
            a_c_in(2, step, far).wait_recv()
    saves = [
        local(kv_w, kv_out),
        local(q_w, wq_out),
        local(o_w, wo_out),
    ]
    span = width // 4

    def project(index, carry):
        cols = pl.ds(pl.multiple_of(index * span, span), span)
        part[:, cols] = matmul_nt(att_ref[...], o_w[cols, :]).astype(jnp.bfloat16)
        return carry

    lax.fori_loop(0, 4, project, 0)
    part_out.start()
    hand_on(1, order[3])
    pass_if(outer, 2)
    pass_if(inner, 3)
    cross(0, order[1])
    hand_on(2, order[1])
    part_out.wait_recv()

    def middle(index, carry):
        at = pl.ds(pl.multiple_of(index * 32, 32), 32)
        there = pl.ds(pl.multiple_of(me_y * own + index * 32, 32), 32)
        values = (
            tok_ref[at, :].astype(jnp.float32)
            + part[there, :].astype(jnp.float32)
            + part_y[at, :].astype(jnp.float32)
        )
        mid_ref[at, :] = values
        scale = lax.rsqrt(jnp.mean(values * values, axis=-1, keepdims=True) + epsilon)
        n2_ref[there, :] = (values * scale * gain_ref[1:2, :]).astype(jnp.bfloat16)
        return carry

    lax.fori_loop(0, own // 32, middle, 0)
    n2_y.start()
    hand_on(2, order[2])
    cross(0, order[2])
    cross(0, order[3])
    hand_on(2, order[3])
    pass_if(outer, 3)
    for kind in (1, 2):
        for index in (1, 2, 3):
            cross(kind, order[index])
    for kind in range(3):
        for step in range(z_size):
            for far in range(2):
                f_c_in(kind, step, far).wait_recv()
    for step in range(z_size):
        d_y_in(step).wait_recv()
    n2_y_in.wait_recv()

    for kind in range(3):
        a_z_done(kind)
    d_z_done()
    tok_y.wait_send()
    part_out.wait_send()
    n2_y.wait_send()
    own_d.wait()
    for copy in saves:
        copy.wait()
    for step in range(z_size):
        d_y(step).wait_send()
        for far in range(2):
            kv_y(step, far).wait_send()
        for kind in range(3):
            if step:
                f_z(kind, step, lambda copy: copy.wait_send())
            a_x(kind, step).wait_send()
            f_x_done(kind, step)
            for far in range(2):
                a_c(kind, step, far).wait_send()
                f_c(kind, step, far).wait_send()


def pre_call(tokens, w_kv, gains, table, segments, cotangent, w_query, w_out, ffn):
    z_size = lax.axis_size("z")
    own, width = tokens.shape
    seq = 2 * own
    rows, cols = w_query.shape
    head = table.shape[2] * 2
    units = ragged_split(ffn[0].shape[1], z_size)[1]
    low = lambda *dims: jax.ShapeDtypeStruct(dims, jnp.bfloat16)
    full = lambda *dims: jax.ShapeDtypeStruct(dims, jnp.float32)
    dma = lambda *lead: pltpu.SemaphoreType.DMA(lead)
    vmem = pl.BlockSpec(memory_space=pltpu.VMEM)
    hbm = pl.BlockSpec(memory_space=pl.ANY)
    wide = lambda *lead: pltpu.VMEM((*lead, width), jnp.bfloat16)
    return pl.pallas_call(
        functools.partial(pre_kernel, z_size),
        out_shape=(
            low(seq, width),
            low(seq, cols),
            low(seq, head),
            low(seq, head),
            low(seq, cols),
            full(own, width),
            low(seq, width),
            full(8, width),
            full(seq, seq),
            low(width, 2 * head + 128),
            low(width, cols),
            low(width, cols),
            low(3, width, units),
            low(z_size, seq, width),
        ),
        in_specs=[vmem] * 5 + [hbm] * 6,
        out_specs=(vmem,) * 9 + (hbm,) * 5,
        scratch_shapes=[
            pltpu.VMEM((width, 2 * head + 128), jnp.bfloat16),
            pltpu.VMEM((width, cols), jnp.bfloat16),
            pltpu.VMEM((width, cols), jnp.bfloat16),
            wide(seq),
            wide(seq),
            wide(own),
            pltpu.VMEM((seq, cols), jnp.float32),
            dma(4),
            dma(4),
            dma(2 * z_size),
            dma(2 * z_size),
            dma(3, z_size + 1),
            dma(3, z_size),
            dma(3, z_size),
            dma(3, z_size),
            dma(3, 2 * z_size),
            dma(3, 2 * z_size),
            dma(3, z_size, 2),
            dma(3, z_size, 2),
            dma(3, z_size),
            dma(3, z_size),
            dma(3, 2 * z_size),
            dma(3, 2 * z_size),
            dma(z_size + 1),
            dma(z_size),
            dma(z_size),
            dma(z_size),
            dma(16),
        ],
        compiler_params=pltpu.CompilerParams(
            collective_id=1, has_side_effects=True, vmem_limit_bytes=VMEM_BYTES
        ),
        cost_estimate=pl.CostEstimate(
            flops=8 * seq * width * cols,
            bytes_accessed=8 * width * (cols + units),
            transcendentals=seq * seq * cols // head,
        ),
    )(tokens, w_kv, gains, table, segments, cotangent, w_query, w_out, *ffn)


def post_kernel(
    z_size,
    main,
    tok_ref,
    gain_ref,
    gain_part_ref,
    n1_ref,
    rot_ref,
    key_ref,
    val_ref,
    att_ref,
    table_ref,
    allow_ref,
    kv_hbm,
    wq_hbm,
    wo_hbm,
    mix_hbm,
    gmf_hbm,
    gmb_hbm,
    mid_hbm,
    sums_hbm,
    mixed_ref,
    tgrad_ref,
    gsum_ref,
    kvg_ref,
    qg_ref,
    og_ref,
    ffn_out,
    kv_w,
    q_w,
    o_w,
    o_part,
    gm,
    gm_f,
    gq,
    gkv,
    kv_sum,
    back_y,
    mix_y,
    mix_z,
    mix_s,
    o_c,
    o_x,
    o_z,
    q_c,
    q_x,
    q_z,
    kv_y,
    kv_c,
    kv_x,
    kv_z,
    gain_own,
    gain_in,
    ffn_in,
    ffn_own,
    load_sem,
    own_sem,
    fx_send,
    fx_recv,
    fz_send,
    fz_recv,
    y_send,
    y_recv,
    my_send,
    my_recv,
    mz_send,
    mz_recv,
    wc_send,
    wc_recv,
    wx_send,
    wx_recv,
    wz_send,
    wz_recv,
    kc_send,
    kc_recv,
    kz_send,
    kz_recv,
    g_send,
    g_recv,
):
    me_z, me_x = lax.axis_index("z"), lax.axis_index("x")
    me_c, me_y = lax.axis_index("c"), lax.axis_index("mp")
    own, width = tok_ref.shape
    seq = 2 * own
    head = key_ref.shape[1]
    cols_here = att_ref.shape[1]
    heads = cols_here // head
    rows = qg_ref.shape[0]
    span = width // z_size
    mine = pl.ds(pl.multiple_of(me_y * own, own), own)
    theirs = pl.ds(pl.multiple_of((1 - me_y) * own, own), own)
    to_y, to_x, to_c = {"mp": 1 - me_y}, {"x": 1 - me_x}, {"c": 1 - me_c}
    head_scale = head ** (-0.5)

    def behind(step):
        return lax.rem(me_z - step + z_size, z_size)

    def to_z(step):
        return {"z": lax.rem(me_z + step, z_size)}

    def row_block(step, x_at, c_at):
        start = ((behind(step) * 2 + x_at) * 2 + c_at) * rows
        return pl.ds(pl.multiple_of(start, rows), rows)

    loads = [
        pltpu.make_async_copy(wo_hbm, o_w, load_sem.at[0]),
        pltpu.make_async_copy(wq_hbm, q_w, load_sem.at[1]),
        pltpu.make_async_copy(
            kv_hbm.at[:, :, :, :, :, pl.ds(0, 2 * head)], kv_w, load_sem.at[2]
        ),
    ]
    for step in range(z_size):
        loads.append(
            pltpu.make_async_copy(mix_hbm.at[step, me_y], mix_s.at[step], load_sem.at[3 + step])
        )
    loads.append(pltpu.make_async_copy(gmf_hbm, gm_f, load_sem.at[3 + z_size]))
    loads.append(pltpu.make_async_copy(gmb_hbm, gm.at[mine], load_sem.at[4 + z_size]))
    mid_load = pltpu.make_async_copy(mid_hbm, gm_f, load_sem.at[5 + z_size])
    for load in loads:
        load.start()

    barrier = pltpu.get_barrier_semaphore()
    peers = [to_y, to_x, to_c] + [to_z(step) for step in range(1, z_size)]
    for where in peers:
        pl.semaphore_signal(barrier, inc=1, device_id=where, device_id_type=MESH_ID)
    pl.semaphore_wait(barrier, len(peers))

    tasks = [(step, kind) for step in (2, 3) for kind in range(3)]

    def f_x(index):
        step, kind = tasks[index]
        return remote(
            sums_hbm.at[kind, step, 1],
            ffn_in.at[index],
            fx_send.at[index],
            fx_recv.at[index],
            to_x,
        )

    def f_own(index):
        step, kind = tasks[index]
        return pltpu.make_async_copy(
            sums_hbm.at[kind, step, 0], ffn_own.at[index % 2], own_sem.at[index % 2]
        )

    def f_z(step, kind, source_z, act):
        for case, columns in (
            ((source_z > 0) & (source_z < z_size - 1), ffn_out.shape[3]),
            ((source_z == 0) | (source_z == z_size - 1), main),
        ):

            @pl.when(case)
            def _(columns=columns):
                cols = pl.ds(0, columns)
                if step == 1:
                    src = sums_hbm.at[kind, 1, 0, :, cols]
                else:
                    src = ffn_in.at[tasks.index((step, kind)), :, cols]
                act(
                    remote(
                        src,
                        ffn_out.at[kind, step, :, cols],
                        fz_send.at[kind, step],
                        fz_recv.at[kind, step],
                        to_z(step),
                    )
                )

    def tick(index):
        step, kind = tasks[index]
        f_x(index).wait_recv()
        f_own(index).wait()
        block = ffn_in.at[index]
        add_rows(block, [ffn_own.at[index % 2]], block, rows)
        if index + 2 < len(tasks):
            f_own(index + 2).start()
        f_z(step, kind, me_z, lambda copy: copy.start())

    def f_x_own(kind):
        return remote(
            sums_hbm.at[kind, 0, 1],
            ffn_out.at[kind, 0],
            fx_send.at[len(tasks) + kind],
            fx_recv.at[len(tasks) + kind],
            to_x,
        )

    f_own(0).start()
    f_own(1).start()
    for index in range(len(tasks)):
        f_x(index).start()
    for kind in range(3):
        f_z(1, kind, me_z, lambda copy: copy.start())

    gm_y = remote(gmb_hbm, gm.at[mine], y_send.at[0], y_recv.at[0], to_y)
    gm_y_in = remote(gm.at[theirs], gm.at[theirs], y_send.at[0], y_recv.at[0], to_y)
    gm_y.start()

    first_z, last_z = (z_size - 1 - me_z) // (z_size - 1), me_z // (z_size - 1)
    inner = first_z + last_z == 0
    order = (
        0,
        1 + (me_z + 1) // 2,
        2 + (2 * me_z - 3) * (1 - first_z - last_z),
        3 - 2 * (me_z // 2),
    )
    right = (None, 1 - me_z // 2, (3 - me_z) * (2 - me_z) // 6 + me_z // 2 * (1 - last_z), 1 - me_z // 2)

    def hop_slot(index):
        step, way = order[index], right[index]
        return way * lax.rem(step + 1, z_size) + (1 - way) * (step - 1 + 4 * ((3 - step) // 2))

    def hop_target(index):
        return {"z": me_z + 2 * right[index] - 1}

    def mix_over_y(step):
        return remote(
            mix_hbm.at[step, 1 - me_y], mix_y.at[step], my_send.at[step], my_recv.at[step], to_y
        )

    def mix_over_z(index):
        slot = hop_slot(index)
        return remote(
            mix_s.at[order[index]],
            mix_z.at[slot],
            mz_send.at[index],
            mz_recv.at[slot],
            hop_target(index),
        )

    def mix_z_in(slot):
        return remote(mix_z.at[slot], mix_z.at[slot], mz_send.at[1], mz_recv.at[slot], to_z(1))

    def mix_add(step, others, last):
        def add_tile(tile, carry):
            at = pl.ds(pl.multiple_of(tile * TILE, TILE), TILE)
            total = mix_s[step, at, :].astype(jnp.float32)
            for other in others:
                total = total + other[at, :].astype(jnp.float32)
            if last:
                mixed_ref[:, at] = (gm_f[:, at] + total.T).astype(jnp.bfloat16)
            else:
                mix_s[step, at, :] = total.astype(jnp.bfloat16)
            return carry

        lax.fori_loop(0, width // TILE, add_tile, 0)

    def mix_step(index):
        step = order[index]
        mix_over_y(step).wait_recv()
        from_y = mix_y.at[step]
        if index:

            @pl.when(inner)
            def _():
                mix_z_in(step).wait_recv()
                mix_add(step, [from_y, mix_z.at[step]], False)

            @pl.when(first_z + last_z > 0)
            def _():
                mix_add(step, [from_y], False)

            mix_over_z(index).start()
        else:
            mid_load.wait()

            @pl.when(first_z == 0)
            def _():
                mix_z_in(0).wait_recv()

            @pl.when(last_z == 0)
            def _():
                mix_z_in(z_size).wait_recv()

            @pl.when(inner)
            def _():
                mix_add(0, [from_y, mix_z.at[0], mix_z.at[z_size]], True)

            @pl.when(first_z > 0)
            def _():
                mix_add(0, [from_y, mix_z.at[z_size]], True)

            @pl.when(last_z > 0)
            def _():
                mix_add(0, [from_y, mix_z.at[0]], True)

    for index in (1, 2, 3, 0):
        mix_over_y(order[index]).start()

    kinds = ((o_part, o_c, o_x, o_z, og_ref), (o_w, q_c, q_x, q_z, qg_ref))

    def w_c(kind, step, far):
        x_at = 1 - me_x if far else me_x
        return remote(
            kinds[kind][0].at[row_block(step, x_at, 1 - me_c)],
            kinds[kind][1].at[step, far],
            wc_send.at[kind, step, far],
            wc_recv.at[kind, step, far],
            to_c,
        )

    def w_x(kind, step):
        return remote(
            kinds[kind][0].at[row_block(step, 1 - me_x, me_c)],
            kinds[kind][2].at[step],
            wx_send.at[kind, step],
            wx_recv.at[kind, step],
            to_x,
        )

    def w_z(kind, index):
        step, slot = order[index], hop_slot(index)
        return remote(
            kinds[kind][0].at[row_block(step, me_x, me_c)],
            kinds[kind][3].at[slot],
            wz_send.at[kind, index],
            wz_recv.at[kind, slot],
            hop_target(index),
        )

    def w_z_in(kind, slot):
        block = kinds[kind][3].at[slot]
        return remote(block, block, wz_send.at[kind, 1], wz_recv.at[kind, slot], to_z(1))

    def w_x_stage(kind, index):
        step = order[index]
        w_c(kind, step, 1).wait_recv()
        block = kinds[kind][0].at[row_block(step, 1 - me_x, me_c)]
        add_rows(block, [kinds[kind][1].at[step, 1]], block, rows)
        w_x(kind, step).start()

    def w_z_stage(kind, index):
        part, from_c, from_x, from_z, result = kinds[kind]
        step = order[index]
        w_c(kind, step, 0).wait_recv()
        w_x(kind, step).wait_recv()
        block = part.at[row_block(step, me_x, me_c)]
        others = [from_c.at[step, 0], from_x.at[step]]
        if index:

            @pl.when(inner)
            def _():
                w_z_in(kind, step).wait_recv()
                add_rows(block, [*others, from_z.at[step]], block, rows)

            @pl.when(first_z + last_z > 0)
            def _():
                add_rows(block, others, block, rows)

            w_z(kind, index).start()
        else:

            @pl.when(first_z == 0)
            def _():
                w_z_in(kind, 0).wait_recv()

            @pl.when(last_z == 0)
            def _():
                w_z_in(kind, z_size).wait_recv()

            @pl.when(inner)
            def _():
                add_rows(block, [*others, from_z.at[0], from_z.at[z_size]], result, rows)

            @pl.when(first_z > 0)
            def _():
                add_rows(block, [*others, from_z.at[z_size]], result, rows)

            @pl.when(last_z > 0)
            def _():
                add_rows(block, [*others, from_z.at[0]], result, rows)

    def w_product(kind, index, left, values):
        step = order[index]
        at = pl.ds(pl.multiple_of(behind(step) * span, 128), span)
        turned = left[:, at].T

        def tile_body(tile, carry):
            cols = pl.ds(pl.multiple_of(tile * TILE, TILE), TILE)
            kinds[kind][0][at, cols] = dot_nn(turned, values[:, cols]).astype(jnp.bfloat16)
            return carry

        lax.fori_loop(0, cols_here // TILE, tile_body, 0)
        for far in (1, 0):
            w_c(kind, step, far).start()

    tick(0)
    tick(1)
    loads[-1].wait()
    gm_y_in.wait_recv()
    w_product(0, 1, gm, att_ref)
    w_product(0, 2, gm, att_ref)
    w_x_stage(0, 1)
    w_product(0, 3, gm, att_ref)
    w_x_stage(0, 2)
    tick(2)
    w_product(0, 0, gm, att_ref)
    w_x_stage(0, 3)
    for load in loads[:-1]:
        load.wait()

    kv_sum[...] = jnp.zeros(kv_sum.shape, jnp.float32)
    table = (table_ref[0], table_ref[1])

    for index in range(2):
        cols = pl.ds(index * (cols_here // 2), cols_here // 2)
        gq[:, cols] = dot_nn(gm[...], o_w[:, cols]).astype(jnp.bfloat16)

    def attend_back(index):
        cols = pl.ds(index * head, head)
        grad_vals = gq[:, cols]
        rotated = rot_ref[:, cols]
        probs = head_probs(rotated, key_ref[...], allow_ref[...])
        grad_probs = matmul_nt(grad_vals, val_ref[...])
        delta = jnp.sum(probs * grad_probs, axis=-1, keepdims=True)
        grad_scores = (probs * (grad_probs - delta)).astype(jnp.bfloat16)
        grad_rot = dot_nn(grad_scores, key_ref[...])
        gq[:, cols] = (spin_back(grad_rot, table) * head_scale).astype(jnp.bfloat16)
        kv_sum[0] += matmul_tn(grad_scores, rotated)
        kv_sum[1] += matmul_tn(probs.astype(jnp.bfloat16), grad_vals)

    for index in range(heads):
        attend_back(index)
        if index == 0:
            w_x_stage(0, 0)
        if 3 + index < len(tasks):
            tick(3 + index)
        if index == heads - 1:
            mix_step(1)
    gkv[:, :head] = spin_back(kv_sum[0], table).astype(jnp.bfloat16)
    gkv[:, head:] = kv_sum[1].astype(jnp.bfloat16)

    w_product(1, 1, n1_ref, gq)
    w_product(1, 2, n1_ref, gq)
    w_x_stage(1, 1)
    w_z_stage(0, 1)
    w_product(1, 3, n1_ref, gq)
    w_x_stage(1, 2)
    w_product(1, 0, n1_ref, gq)
    w_x_stage(1, 3)
    w_x_stage(1, 0)
    for kind in range(3):
        f_x_own(kind).start()

    gm_y.wait_send()
    back = gm
    def input_tile(index, carry):
        at = pl.ds(pl.multiple_of(index * span, 128), span)
        back[:, at] = (
            matmul_nt(gq[...], q_w[at, :]) + matmul_nt(gkv[...], kv_w[index].reshape(span, 2 * head))
        ).astype(jnp.bfloat16)
        return carry

    lax.fori_loop(0, z_size, input_tile, 0)
    back_out = remote(back.at[theirs], back_y, y_send.at[1], y_recv.at[1], to_y)
    back_out.start()

    kv_part = kv_w

    def kv_tile(index, carry):
        at = pl.ds(pl.multiple_of(index * span, 128), span)
        product = dot_nn(n1_ref[:, at].T, gkv[...]).astype(jnp.bfloat16)
        kv_part[index] = product.reshape(kv_part.shape[1:])
        return carry

    lax.fori_loop(0, z_size, kv_tile, 0)
    kv_over_y = remote(kv_part.at[:, :, :, 1 - me_y], kv_y, y_send.at[2], y_recv.at[2], to_y)
    kv_over_y.start()
    mix_step(2)
    w_z_stage(0, 2)
    mix_step(3)
    w_z_stage(0, 3)

    back_out.wait_recv()

    def input_rows(index, total):
        at = pl.ds(pl.multiple_of(index * 32, 32), 32)
        there = pl.ds(pl.multiple_of(me_y * own + index * 32, 32), 32)
        upstream = back[there, :].astype(jnp.float32) + back_y[at, :].astype(jnp.float32)
        grad, gain_part = norm_back(
            tok_ref[at, :].astype(jnp.float32), gain_ref[0:1, :], upstream
        )
        tgrad_ref[at, :] = (gm_f[at, :] + grad).astype(jnp.bfloat16)
        return total + gain_part

    attn_gain_part = lax.fori_loop(
        0, own // 32, input_rows, jnp.zeros((1, width), jnp.float32)
    )
    for index in range(4):
        at = slice(index * span, (index + 1) * span)
        gain_own[0, index : index + 1, :] = attn_gain_part[:, at]
        gain_own[0, 4 + index : 5 + index, :] = gain_part_ref[4 + index : 5 + index, :]

    def gain_send(stage, where):
        return remote(
            gain_own.at[stage], gain_in.at[stage], g_send.at[stage], g_recv.at[stage], where
        )

    gain_hops = [gain_send(0, to_y), gain_send(1, to_c), gain_send(2, to_x)]
    gain_last = [
        remote(
            gain_own.at[3], gain_in.at[2 + step], g_send.at[2 + step], g_recv.at[2 + step], to_z(step)
        )
        for step in range(1, z_size)
    ]

    def gain_fold(stage):
        gain_hops[stage].wait_recv()
        gain_own[stage + 1] = gain_own[stage] + gain_in[stage]

    gain_hops[0].start()
    mid_load.start()
    w_z_stage(1, 1)
    w_z_stage(0, 0)
    w_z_stage(1, 2)
    gain_fold(0)
    gain_hops[1].start()
    mix_step(0)
    w_z_stage(1, 3)
    gain_fold(1)
    gain_hops[2].start()
    kv_over_y.wait_recv()

    def kv_add_y(index, carry):
        for x_at in range(2):
            for c_at in range(2):
                block = kv_part.at[index, x_at, c_at, me_y]
                block[...] = (
                    block[...].astype(jnp.float32) + kv_y[index, x_at, c_at].astype(jnp.float32)
                ).astype(jnp.bfloat16)
        return carry

    lax.fori_loop(0, z_size, kv_add_y, 0)
    kv_over_c = remote(
        kv_part.at[:, :, 1 - me_c, me_y], kv_c, kc_send.at[0], kc_recv.at[0], to_c
    )
    kv_over_c.start()
    gain_fold(2)
    for copy in gain_last:
        copy.start()
    kv_over_c.wait_recv()

    def kv_add_c(index, carry):
        for x_at in range(2):
            block = kv_part.at[index, x_at, me_c, me_y]
            block[...] = (
                block[...].astype(jnp.float32) + kv_c[index, x_at].astype(jnp.float32)
            ).astype(jnp.bfloat16)
        return carry

    lax.fori_loop(0, z_size, kv_add_c, 0)
    kv_over_x = remote(
        kv_part.at[:, 1 - me_x, me_c, me_y], kv_x, kc_send.at[1], kc_recv.at[1], to_x
    )
    kv_over_x.start()
    w_z_stage(1, 0)
    kv_over_x.wait_recv()

    def kv_add_x(index, carry):
        block = kv_part.at[index, me_x, me_c, me_y]
        block[...] = (
            block[...].astype(jnp.float32) + kv_x[index].astype(jnp.float32)
        ).astype(jnp.bfloat16)
        return carry

    lax.fori_loop(0, z_size, kv_add_x, 0)
    kv_over_z = [
        remote(
            kv_part.at[lax.rem(me_z + step, z_size), me_x, me_c, me_y],
            kv_z.at[step - 1],
            kz_send.at[step],
            kz_recv.at[step],
            to_z(step),
        )
        for step in range(1, z_size)
    ]
    for copy in kv_over_z:
        copy.start()
    for copy in gain_last:
        copy.wait_recv()
    gsum_ref[...] = gain_own[3] + gain_in[3] + gain_in[4] + gain_in[5]
    for copy in kv_over_z:
        copy.wait_recv()
    kvg_ref[...] = (
        kv_part[me_z, me_x, me_c, me_y].astype(jnp.float32)
        + kv_z[0].astype(jnp.float32)
        + kv_z[1].astype(jnp.float32)
        + kv_z[2].astype(jnp.float32)
    )

    back_out.wait_send()
    kv_over_y.wait_send()
    kv_over_c.wait_send()
    kv_over_x.wait_send()
    for kind in range(3):
        f_x_own(kind).wait()
    for index in range(len(tasks)):
        f_x(index).wait_send()
    for step in range(1, z_size):
        for kind in range(3):
            f_z(step, kind, me_z, lambda copy: copy.wait_send())
            f_z(step, kind, behind(step), lambda copy: copy.wait_recv())
    for copy in gain_hops + gain_last + kv_over_z:
        copy.wait_send()
    for step in range(z_size):
        mix_over_y(step).wait_send()
        if step:
            mix_over_z(step).wait_send()
        for kind in range(2):
            w_c(kind, step, 0).wait_send()
            w_c(kind, step, 1).wait_send()
            w_x(kind, step).wait_send()
            if step:
                w_z(kind, step).wait_send()


def post_call(
    tokens,
    gains,
    gain_part,
    normed_one,
    rotated,
    keys,
    values,
    attn_vals,
    table,
    allowed,
    kv_weight,
    query_weight,
    out_weight,
    mix_parts,
    grad_mid,
    grad_mid_low,
    mid,
    ffn_sums,
    main,
):
    z_size = lax.axis_size("z")
    own, width = tokens.shape
    seq = 2 * own
    head = keys.shape[1]
    cols = attn_vals.shape[1]
    rows = width // (4 * z_size)
    units = ffn_sums.shape[4]
    low = lambda *dims: pltpu.VMEM(dims, jnp.bfloat16)
    full = lambda *dims: pltpu.VMEM(dims, jnp.float32)
    out_full = lambda *dims: jax.ShapeDtypeStruct(dims, jnp.float32)
    out_low = lambda *dims: jax.ShapeDtypeStruct(dims, jnp.bfloat16)
    dma = lambda *lead: pltpu.SemaphoreType.DMA(lead)
    vmem = pl.BlockSpec(memory_space=pltpu.VMEM)
    hbm = pl.BlockSpec(memory_space=pl.ANY)
    z = z_size
    return pl.pallas_call(
        functools.partial(post_kernel, z_size, main),
        out_shape=(
            out_low(own, width),
            out_low(own, width),
            out_full(8, width // z),
            out_full(rows // 2, 2 * head),
            out_full(rows, cols),
            out_full(rows, cols),
            out_low(3, z, rows, units),
        ),
        in_specs=[vmem] * 10 + [hbm] * 8,
        out_specs=(vmem,) * 6 + (hbm,),
        scratch_shapes=[
            low(z, 2, 2, 2, rows // 2, 2 * head),
            low(width, cols),
            low(width, cols),
            low(width, cols),
            low(seq, width),
            full(own, width),
            low(seq, cols),
            low(seq, 2 * head),
            full(2, seq, head),
            low(own, width),
            low(z, width, own),
            low(z + 1, width, own),
            low(z, width, own),
            low(z, 2, rows, cols),
            low(z, rows, cols),
            low(z + 1, rows, cols),
            low(z, 2, rows, cols),
            low(z, rows, cols),
            low(z + 1, rows, cols),
            low(z, 2, 2, rows // 2, 2 * head),
            low(z, 2, rows // 2, 2 * head),
            low(z, rows // 2, 2 * head),
            low(z - 1, rows // 2, 2 * head),
            full(4, 8, width // z),
            full(6, 8, width // z),
            low(6, rows, units),
            low(2, rows, units),
            dma(6 + z),
            dma(2),
            dma(9),
            dma(9),
            dma(3, z),
            dma(3, z),
            dma(3),
            dma(3),
            dma(z),
            dma(z),
            dma(z),
            dma(z + 1),
            dma(2, z, 2),
            dma(2, z, 2),
            dma(2, z),
            dma(2, z),
            dma(2, z),
            dma(2, z + 1),
            dma(2),
            dma(2),
            dma(z),
            dma(z),
            dma(6),
            dma(6),
        ],
        compiler_params=pltpu.CompilerParams(
            collective_id=2, has_side_effects=True, vmem_limit_bytes=VMEM_BYTES
        ),
        cost_estimate=pl.CostEstimate(
            flops=14 * seq * width * cols,
            bytes_accessed=10 * width * cols,
            transcendentals=seq * seq * cols // head,
        ),
    )(
        tokens,
        gains,
        gain_part,
        normed_one,
        rotated,
        keys,
        values,
        attn_vals,
        table,
        allowed,
        kv_weight.reshape(z, 2, 2, 2, rows // 2, kv_weight.shape[1]),
        query_weight,
        out_weight,
        mix_parts,
        grad_mid,
        grad_mid_low,
        mid,
        ffn_sums,
    )


def layout_kernel(
    z_size,
    main,
    sum_ref,
    ffn_ref,
    q_ref,
    o_ref,
    kv_ref,
    mixed_in,
    tgrad_in,
    wg_ref,
    wu_ref,
    wd_ref,
    qg_ref,
    og_ref,
    kvg_ref,
    mixed_ref,
    tgrad_ref,
):
    me_z = lax.axis_index("z")
    for kind, out in enumerate((wg_ref, wu_ref, wd_ref)):
        for step in range(z_size):
            at = lax.rem(me_z - step + z_size, z_size)
            values = ffn_ref[kind, step].astype(jnp.float32)
            if step == 0:
                values = values + sum_ref[kind, 0, 0].astype(jnp.float32)
            body = pl.ds(pl.multiple_of(at * main, 128), main)
            out[:, body] = values[:, :main]

            @pl.when((at > 0) & (at < z_size - 1))
            def _(out=out, at=at, values=values):
                tail = z_size * main + lax.rem(at + 1, 2) * 128
                out[:, pl.ds(pl.multiple_of(tail, 128), 128)] = values[:, main:]
    qg_ref[...] = q_ref[...]
    og_ref[...] = o_ref[...]
    kvg_ref[...] = kv_ref[...]
    mixed_ref[...] = mixed_in[...]
    tgrad_ref[...] = tgrad_in[...]


def layout_call(ffn_sums, ffn_grads, query_grad, out_grad, kv_grad, mixed, tokens_grad, ffn_cols):
    z_size = lax.axis_size("z")
    main, units = ragged_split(ffn_cols, z_size)
    rows, cols = query_grad.shape
    parts = rows // 32
    kv_rows = kv_grad.shape[0] // parts
    full = lambda *dims: jax.ShapeDtypeStruct(dims, jnp.float32)
    row = lambda height, width: pl.BlockSpec((height, width), lambda index: (index, 0))
    own, width = mixed.shape
    share = pl.BlockSpec((own, width // parts), lambda index: (0, index))
    specs = [row(32, cols), row(32, cols), row(kv_rows, kv_grad.shape[1]), share, share]
    return pl.pallas_call(
        functools.partial(layout_kernel, z_size, main),
        grid=(parts,),
        out_shape=(
            *[full(rows, ffn_cols)] * 3,
            full(rows, cols),
            full(rows, cols),
            full(*kv_grad.shape),
            jax.ShapeDtypeStruct(mixed.shape, jnp.bfloat16),
            jax.ShapeDtypeStruct(mixed.shape, jnp.bfloat16),
        ),
        in_specs=[
            pl.BlockSpec((3, 1, 1, 32, units), lambda index: (0, 0, 0, index, 0)),
            pl.BlockSpec((3, z_size, 32, units), lambda index: (0, 0, index, 0)),
            *specs,
        ],
        out_specs=(*[row(32, ffn_cols)] * 3, *specs),
        compiler_params=pltpu.CompilerParams(vmem_limit_bytes=VMEM_BYTES),
    )(ffn_sums, ffn_grads, query_grad, out_grad, kv_grad, mixed, tokens_grad)


FF_SPLIT = 4


def ffn_pass(normed, grad_out, gate_weight, up_weight, down_weight):
    gate = jnp.dot(normed, gate_weight, preferred_element_type=jnp.float32)
    up_proj = jnp.dot(normed, up_weight, preferred_element_type=jnp.float32)
    grad_hidden = jnp.dot(grad_out, down_weight, preferred_element_type=jnp.float32)
    product, pull = jax.vjp(gelu_product, gate, up_proj)
    hidden = product.astype(jnp.bfloat16)
    grad_gate_f, grad_up_f = pull(grad_hidden)
    grad_gate = grad_gate_f.astype(jnp.bfloat16)
    grad_up = grad_up_f.astype(jnp.bfloat16)
    mixed_part = matmul_nt(hidden, down_weight).astype(jnp.bfloat16)
    normed_part = (matmul_nt(grad_gate, gate_weight) + matmul_nt(grad_up, up_weight)).astype(
        jnp.bfloat16
    )
    weight_parts = [
        matmul_tn(normed, grad_gate).astype(jnp.bfloat16),
        matmul_tn(normed, grad_up).astype(jnp.bfloat16),
        matmul_tn(grad_out, hidden).astype(jnp.bfloat16),
    ]
    return mixed_part, normed_part, weight_parts


def shards_general(
    tokens,
    segments,
    positions,
    cotangent,
    attn_gain,
    ffn_gain,
    w_kv,
    w_query,
    w_out,
    w_gate,
    w_up,
    w_down,
):
    everywhere = ("z", "xc", "mp")
    dp = ("z", "xc")
    z_size = lax.axis_size("z")
    xc_size = lax.axis_size("xc")
    gains = lax.all_gather(
        jnp.stack([attn_gain, ffn_gain], axis=1), everywhere, axis=0, tiled=True
    ).astype(jnp.float32)
    gain_one, gain_two = gains[:, 0], gains[:, 1]
    kv_weight = lax.all_gather(w_kv, everywhere, axis=0, tiled=True)
    head_dim = kv_weight.shape[1] // 2
    width = tokens.shape[1]
    seq_len = segments.shape[0]
    heads_here = w_query.shape[1] // head_dim
    scale = head_dim ** (-0.5)
    cosine, sine = rotary_angles(positions, head_dim)
    inputs_f = tokens.astype(jnp.float32)
    tokens_all = lax.all_gather(tokens, "mp", axis=0, tiled=True)
    normed_one = norm_gain(tokens_all.astype(jnp.float32), gain_one).astype(jnp.bfloat16)
    query_weight = lax.all_gather(w_query, dp, axis=0, tiled=True)
    out_weight = lax.all_gather(w_out, dp, axis=0, tiled=True)

    rows = w_gate.shape[0]
    unit = w_gate.shape[1] // z_size

    def spread(weight):
        pieces = weight.reshape(rows, z_size, unit).transpose(1, 0, 2)
        pieces = lax.all_to_all(pieces, "z", split_axis=0, concat_axis=0, tiled=True)
        return lax.all_gather(pieces, "xc", axis=1, tiled=False).reshape(width, unit)

    gate_weight, up_weight, down_weight = spread(w_gate), spread(w_up), spread(w_down)
    grad_all = lax.all_gather(cotangent, ("z", "mp"), axis=0, tiled=True)

    query = jnp.dot(normed_one, query_weight, preferred_element_type=jnp.float32).reshape(
        seq_len, heads_here, head_dim
    )
    rotated = (rotate(query, cosine[:, None], sine[:, None]) * scale).astype(jnp.bfloat16)
    keyval = jnp.dot(normed_one, kv_weight, preferred_element_type=jnp.float32)
    keys = rotate(keyval[:, :head_dim], cosine, sine).astype(jnp.bfloat16)
    values = keyval[:, head_dim:].astype(jnp.bfloat16)
    allowed = block_allowed(segments, 0, seq_len)
    scores = jnp.einsum("thd,sd->hts", rotated, keys, preferred_element_type=jnp.float32)
    scores = jnp.where(allowed[None], scores, masked_score)
    row_max = jnp.max(scores, axis=-1, keepdims=True)
    weights = jnp.exp(scores - row_max)
    probs = weights / jnp.sum(weights, axis=-1, keepdims=True)
    probs_low = probs.astype(jnp.bfloat16)
    attn_vals = (
        jnp.einsum("hts,sd->thd", probs_low, values, preferred_element_type=jnp.float32)
        .reshape(seq_len, heads_here * head_dim)
        .astype(jnp.bfloat16)
    )
    mid = inputs_f + lax.psum_scatter(
        matmul_nt(attn_vals, out_weight).astype(jnp.bfloat16),
        "mp",
        scatter_dimension=0,
        tiled=True,
    ).astype(jnp.float32)
    normed_two = norm_gain(mid, gain_two).astype(jnp.bfloat16)
    normed_all = lax.all_gather(normed_two, ("z", "mp"), axis=0, tiled=True)

    mixed_part, normed_part, weight_parts = ffn_pass(
        normed_all, grad_all, gate_weight, up_weight, down_weight
    )
    grad_normed_two = lax.psum_scatter(
        normed_part, ("z", "mp"), scatter_dimension=0, tiled=True
    ).astype(jnp.float32)
    mixed = (
        mid
        + lax.psum_scatter(mixed_part, ("z", "mp"), scatter_dimension=0, tiled=True).astype(
            jnp.float32
        )
    ).astype(jnp.bfloat16)

    def collect(part):
        pieces = part.reshape(z_size, xc_size, rows, unit).transpose(1, 0, 2, 3)
        pieces = pieces.reshape(xc_size * z_size * rows, unit)
        pieces = lax.psum_scatter(pieces, "xc", scatter_dimension=0, tiled=True)
        pieces = pieces.reshape(z_size, rows, unit)
        pieces = lax.all_to_all(pieces, "z", split_axis=0, concat_axis=0, tiled=True)
        return pieces.transpose(1, 0, 2).reshape(rows, z_size * unit).astype(jnp.float32)

    w_gate_grad, w_up_grad, w_down_grad = [collect(part) for part in weight_parts]

    norm_pull_two = jax.vjp(norm_gain, mid, gain_two)[1]
    grad_mid_norm, grad_gain_two = norm_pull_two(grad_normed_two)
    grad_mid = cotangent.astype(jnp.float32) + grad_mid_norm
    grad_mid_all = lax.all_gather(grad_mid.astype(jnp.bfloat16), "mp", axis=0, tiled=True)
    grad_vals = (
        jnp.dot(grad_mid_all, out_weight, preferred_element_type=jnp.float32)
        .astype(jnp.bfloat16)
        .reshape(seq_len, heads_here, head_dim)
    )
    grad_probs = jnp.einsum("thd,sd->hts", grad_vals, values, preferred_element_type=jnp.float32)
    delta = jnp.sum(probs * grad_probs, axis=-1, keepdims=True)
    grad_scores = (probs * (grad_probs - delta)).astype(jnp.bfloat16)
    grad_rot = jnp.einsum("hts,sd->thd", grad_scores, keys, preferred_element_type=jnp.float32)
    key_sum = jnp.einsum("hts,thd->sd", grad_scores, rotated, preferred_element_type=jnp.float32)
    value_sum = jnp.einsum("hts,thd->sd", probs_low, grad_vals, preferred_element_type=jnp.float32)
    grad_query = (
        (unrotate(grad_rot, cosine[:, None], sine[:, None]) * scale)
        .reshape(seq_len, heads_here * head_dim)
        .astype(jnp.bfloat16)
    )
    grad_kv = jnp.concatenate([unrotate(key_sum, cosine, sine), value_sum], axis=1).astype(
        jnp.bfloat16
    )
    grad_normed_one = lax.psum_scatter(
        (matmul_nt(grad_query, query_weight) + matmul_nt(grad_kv, kv_weight)).astype(jnp.bfloat16),
        "mp",
        scatter_dimension=0,
        tiled=True,
    ).astype(jnp.float32)
    norm_pull_one = jax.vjp(norm_gain, inputs_f, gain_one)[1]
    grad_input_norm, grad_gain_one = norm_pull_one(grad_normed_one)
    tokens_grad = (grad_mid + grad_input_norm).astype(jnp.bfloat16)

    w_query_grad = lax.psum_scatter(
        matmul_tn(normed_one, grad_query).astype(jnp.bfloat16), dp, scatter_dimension=0, tiled=True
    ).astype(jnp.float32)
    w_out_grad = lax.psum_scatter(
        matmul_tn(grad_mid_all, attn_vals).astype(jnp.bfloat16), dp, scatter_dimension=0, tiled=True
    ).astype(jnp.float32)
    small = jnp.concatenate(
        [matmul_tn(normed_one, grad_kv), grad_gain_one[:, None], grad_gain_two[:, None]], axis=1
    )
    small = lax.psum_scatter(small, everywhere, scatter_dimension=0, tiled=True)
    kv_grad = small[:, : 2 * head_dim]
    return (
        mixed,
        tokens_grad,
        small[:, 2 * head_dim],
        small[:, 2 * head_dim + 1],
        kv_grad,
        w_query_grad,
        w_out_grad,
        w_gate_grad,
        w_up_grad,
        w_down_grad,
    )


def shards_fast(
    tokens,
    segments,
    positions,
    cotangent,
    attn_gain,
    ffn_gain,
    w_kv,
    w_query,
    w_out,
    w_gate,
    w_up,
    w_down,
):
    seq_len = segments.shape[0]
    cosine, sine = rotary_angles(positions, w_kv.shape[1] // 2)
    table = jnp.stack(
        [
            jnp.concatenate([cosine, cosine], axis=1),
            jnp.concatenate([-sine, sine], axis=1),
        ]
    )
    gain_rows = jnp.pad(
        jnp.stack([attn_gain, ffn_gain]).astype(jnp.float32),
        ((0, 6), (0, 128 - attn_gain.shape[0])),
    )
    segment_rows = jnp.broadcast_to(segments.astype(jnp.float32)[None, :], (8, seq_len))
    (
        normed_one,
        rotated,
        keys,
        values,
        attn_vals,
        mid,
        normed_two,
        gains,
        allowed,
        kv_weight,
        query_weight,
        out_weight,
        ffn_weights,
        grad_all,
    ) = pre_call(
        tokens,
        w_kv,
        gain_rows,
        table,
        segment_rows,
        cotangent,
        w_query,
        w_out,
        (w_gate, w_up, w_down),
    )
    main = ragged_split(w_gate.shape[1], lax.axis_size("z"))[0]
    grad_mid, gain_part, mix_parts, ffn_sums, grad_mid_low = ffn_call(
        gains, normed_two, grad_all, ffn_weights, mid, w_gate.shape[0], main
    )
    mixed, tokens_grad, gain_grads, kv_grad, query_grad, out_grad, ffn_grads = post_call(
        tokens,
        gains,
        gain_part,
        normed_one,
        rotated,
        keys,
        values,
        attn_vals,
        table,
        allowed,
        kv_weight,
        query_weight,
        out_weight,
        mix_parts,
        grad_mid,
        grad_mid_low,
        mid,
        ffn_sums,
        main,
    )
    *ffn_out, query_grad, out_grad, kv_grad, mixed, tokens_grad = layout_call(
        ffn_sums,
        ffn_grads,
        query_grad,
        out_grad,
        kv_grad,
        mixed,
        tokens_grad,
        w_gate.shape[1],
    )
    share = attn_gain.shape[0]
    place = lax.axis_index(("z", "x", "c", "mp")) * share
    gain_grads = gain_grads.reshape(2, gain_grads.size // 2)
    gain_grads = lax.dynamic_slice(gain_grads, (0, place), (2, share))
    return (
        mixed,
        tokens_grad,
        gain_grads[0],
        gain_grads[1],
        kv_grad,
        query_grad,
        out_grad,
        *ffn_out,
    )


def solution(mesh):
    dp_size, mp_size = mesh.shape["dp"], mesh.shape["mp"]
    if dp_size == 4 * FF_SPLIT and mp_size == 2:
        body, dp = shards_fast, ("z", "x", "c")
        sizes = (FF_SPLIT, 2, 2, mp_size)
    else:
        body, dp = shards_general, ("z", "xc")
        sizes = (FF_SPLIT, dp_size // FF_SPLIT, mp_size)
    all_axes = (*dp, "mp")
    fine = jax.sharding.Mesh(mesh.devices.reshape(sizes), all_axes)
    in_specs = (
        P(all_axes, None),
        P(dp),
        P(dp),
        P(all_axes, None),
        P(all_axes),
        P(all_axes),
        P(all_axes, None),
        P(dp, "mp"),
        P(dp, "mp"),
        P(dp, "mp"),
        P(dp, "mp"),
        P(dp, "mp"),
    )
    out_specs = (
        P(all_axes, None),
        P(all_axes, None),
        P(all_axes),
        P(all_axes),
        P(all_axes, None),
        P(dp, "mp"),
        P(dp, "mp"),
        P(dp, "mp"),
        P(dp, "mp"),
        P(dp, "mp"),
    )
    return jax.shard_map(body, mesh=fine, in_specs=in_specs, out_specs=out_specs, check_vma=False)
```

```python
import functools

import jax
import jax.numpy as jnp
from jax import lax
from jax.experimental import pallas as pl
from jax.experimental.pallas import tpu as pltpu
from jax.sharding import PartitionSpec as P

WINDOW = 2048


epsilon = 1e-06
rope_base = 10000.0
masked_score = -1e30
VMEM_BYTES = 66_000_000


def norm_gain(values, gain):
    return values * lax.rsqrt(jnp.mean(values * values, axis=-1, keepdims=True) + epsilon) * gain


def rotary_angles(positions, head_width):
    quarter = head_width // 4
    freqs = rope_base ** (-jnp.arange(quarter).astype(jnp.float32) / quarter)
    phase = positions.astype(jnp.float32)[:, None] * freqs[None, :]
    return (jnp.cos(phase), jnp.sin(phase))


def rotate(values, cosine, sine):
    quarter = cosine.shape[-1]
    first_half = values[..., :quarter]
    second_half = values[..., quarter : 2 * quarter]
    return jnp.concatenate(
        [
            first_half * cosine - second_half * sine,
            second_half * cosine + first_half * sine,
            values[..., 2 * quarter :],
        ],
        axis=-1,
    )


def unrotate(values, cosine, sine):
    quarter = cosine.shape[-1]
    first_half = values[..., :quarter]
    second_half = values[..., quarter : 2 * quarter]
    return jnp.concatenate(
        [
            first_half * cosine + second_half * sine,
            second_half * cosine - first_half * sine,
            values[..., 2 * quarter :],
        ],
        axis=-1,
    )


def gelu_product(gate, up_proj):
    return jax.nn.gelu(gate, approximate=True) * up_proj


def matmul_nt(left, right):
    return lax.dot_general(
        left, right, (((1,), (1,)), ((), ())), preferred_element_type=jnp.float32
    )


def matmul_tn(left, right):
    return lax.dot_general(
        left, right, (((0,), (0,)), ((), ())), preferred_element_type=jnp.float32
    )


def block_allowed(segments, first_row, rows):
    seq_len = segments.shape[0]
    query_rows = first_row + jnp.arange(rows)
    key_rows = jnp.arange(seq_len)
    return (
        (segments[:, None] == segments[None, :])
        & (key_rows[None, :] <= query_rows[:, None])
        & (query_rows[:, None] - key_rows[None, :] < WINDOW)
    )


MESH_ID = pl.DeviceIdType.MESH
GELU_A = 0.7978845608028654
GELU_B = 0.044715
TILE = 256
WIDE = 512


def remote(src, dst, send_sem, recv_sem, where):
    return pltpu.make_async_remote_copy(
        src_ref=src,
        dst_ref=dst,
        send_sem=send_sem,
        recv_sem=recv_sem,
        device_id=where,
        device_id_type=MESH_ID,
    )


class Halves:
    def __init__(self, src, dst, send_sem, recv_sem, where):
        rows = src.shape[0] // 2
        cuts = [pl.ds(part * rows, rows) for part in range(2)]
        self.copies = [
            remote(src.at[cut], dst.at[cut], send_sem.at[part], recv_sem.at[part], where)
            for part, cut in enumerate(cuts)
        ]

    def start(self):
        for copy in self.copies:
            copy.start()

    def wait_recv(self):
        for copy in self.copies:
            copy.wait_recv()

    def wait_send(self):
        for copy in self.copies:
            copy.wait_send()


def dot_nn(left, right):
    return lax.dot_general(
        left, right, (((1,), (0,)), ((), ())), preferred_element_type=jnp.float32
    )


def gelu_parts(gate):
    square = gate * gate
    bend = jnp.tanh(GELU_A * gate * (1.0 + GELU_B * square))
    half = 0.5 * (1.0 + bend)
    slope = half + 0.5 * gate * (1.0 - bend * bend) * GELU_A * (1.0 + 3.0 * GELU_B * square)
    return gate * half, slope


def add_rows(first, rest, out, count):
    def body(index, carry):
        step = pl.ds(pl.multiple_of(index * 32, 32), 32)
        total = first[step, :].astype(jnp.float32)
        for other in rest:
            total = total + other[step, :].astype(jnp.float32)
        out[step, :] = total.astype(out.dtype)
        return carry

    lax.fori_loop(0, count // 32, body, 0)


def norm_back(values, gain, upstream):
    scale = lax.rsqrt(jnp.mean(values * values, axis=-1, keepdims=True) + epsilon)
    normed = values * scale
    pulled = gain * upstream
    back = scale * (pulled - normed * jnp.mean(normed * pulled, axis=-1, keepdims=True))
    return back, jnp.sum(upstream * normed, axis=0, keepdims=True)


def ffn_kernel(
    z_size,
    main,
    gain_ref,
    own_hbm,
    dy_hbm,
    w_hbm,
    mid_hbm,
    gm_ref,
    gain_part,
    mix_hbm,
    sums_hbm,
    gm_hbm,
    n2,
    dy,
    w3,
    h3,
    n2_t,
    dy_t,
    gn_part,
    mix_buf,
    gn_y,
    gn_z,
    gn_s,
    c_in,
    x_in,
    mid,
    load_sem,
    mix_sem,
    ag_y_send,
    ag_y_recv,
    ag_z_send,
    ag_z_recv,
    rs_y_send,
    rs_y_recv,
    rs_z_send,
    rs_z_recv,
    c_send,
    c_recv,
    x_send,
    x_recv,
    out_sem,
):
    own = own_hbm.shape[0] // 2
    width = own_hbm.shape[1]
    units = w3.shape[2]
    rows = c_in.shape[3]
    span = width // z_size
    me_y, me_z = lax.axis_index("mp"), lax.axis_index("z")
    me_x, me_c = lax.axis_index("x"), lax.axis_index("c")
    mine = pl.ds(pl.multiple_of(me_y * own, own), own)
    theirs = pl.ds(pl.multiple_of((1 - me_y) * own, own), own)
    to_y, to_x, to_c = {"mp": 1 - me_y}, {"x": 1 - me_x}, {"c": 1 - me_c}

    def ahead(step):
        return lax.rem(me_z + step, z_size)

    def to_z(step):
        return {"z": ahead(step)}

    def row_block(z_at, x_at, c_at):
        return pl.ds(pl.multiple_of(((z_at * 2 + x_at) * 2 + c_at) * rows, rows), rows)

    inner = (me_z > 0) & (me_z < z_size - 1)
    outer = (me_z == 0) | (me_z == z_size - 1)

    def w_load(index, columns):
        cols = pl.ds(0, columns)
        return pltpu.make_async_copy(
            w_hbm.at[index, :, cols], w3.at[index, :, cols], load_sem.at[z_size + index]
        )

    def w_loads(act):
        for case, columns in ((inner, units), (outer, main)):

            @pl.when(case)
            def _(columns=columns):
                for index in range(3):
                    act(w_load(index, columns))

    w_loads(lambda copy: copy.start())
    dy_loads = [
        pltpu.make_async_copy(dy_hbm.at[index], dy, load_sem.at[index])
        for index in range(z_size)
    ]
    own_load = pltpu.make_async_copy(own_hbm, n2.at[0], load_sem.at[z_size + 3])
    mid_load = pltpu.make_async_copy(mid_hbm, mid, load_sem.at[z_size + 4])
    for load in (own_load, dy_loads[0], mid_load):
        load.start()

    barrier = pltpu.get_barrier_semaphore()
    peers = [to_y, to_x, to_c] + [to_z(step) for step in range(1, z_size)]
    for where in peers:
        pl.semaphore_signal(barrier, inc=1, device_id=where, device_id_type=MESH_ID)
    pl.semaphore_wait(barrier, len(peers))

    def ag_y(index):
        block = n2.at[index, mine]
        return Halves(block, block, ag_y_send.at[index], ag_y_recv.at[index], to_y)

    def ag_y_in(index):
        block = n2.at[index, theirs]
        return Halves(block, block, ag_y_send.at[index], ag_y_recv.at[index], to_y)

    def ag_z(index):
        src = own_hbm.at[mine] if index == 0 else n2.at[index, mine]
        return Halves(
            src, n2.at[index + 1, mine], ag_z_send.at[index], ag_z_recv.at[index + 1], to_z(1)
        )

    def ag_z_in(index):
        block = n2.at[index, mine]
        return Halves(block, block, ag_z_send.at[0], ag_z_recv.at[index], to_z(1))

    def ag_last():
        return Halves(
            n2.at[2, theirs], n2.at[3, theirs], ag_y_send.at[3], ag_y_recv.at[3], to_z(1)
        )

    def forward(index):
        ag_z_in(index).wait_recv()
        ag_z(index).start()
        ag_y(index).start()

    ag_z(0).start()

    mix_copies = []

    def turn(source, target, index):
        def turn_tile(tile, carry):
            at = pl.ds(pl.multiple_of(tile * span, 128), span)
            target[at, pl.ds(index * 2 * own, 2 * own)] = source[:, at].T
            return carry

        lax.fori_loop(0, z_size, turn_tile, 0)

    def chunk(index):
        if index:
            mix_copies[index - 1].wait()
        dy_loads[index].wait()
        rows_at = pl.ds(index * 2 * own, 2 * own)

        def up_tile(tile, carry):
            cols = pl.ds(pl.multiple_of(tile * WIDE, WIDE), WIDE)
            gate = dot_nn(n2[index], w3[0, :, cols])
            up_proj = dot_nn(n2[index], w3[1, :, cols])
            grad_hidden = dot_nn(dy[...], w3[2, :, cols])
            act, slope = gelu_parts(gate)
            h3[0, rows_at, cols] = (grad_hidden * up_proj * slope).astype(jnp.bfloat16)
            h3[1, rows_at, cols] = (grad_hidden * act).astype(jnp.bfloat16)
            h3[2, rows_at, cols] = (act * up_proj).astype(jnp.bfloat16)
            return carry

        lax.fori_loop(0, units // WIDE, up_tile, 0)

        def down_tile(tile, carry):
            at = pl.ds(pl.multiple_of(tile * span, 128), span)
            normed = matmul_nt(w3[0, at, :], h3[0, rows_at, :]) + matmul_nt(
                w3[1, at, :], h3[1, rows_at, :]
            )
            mixed = matmul_nt(w3[2, at, :], h3[2, rows_at, :])
            for half in range(2):
                cols = slice(half * own, (half + 1) * own)
                gn_part[index, half, at, :] = normed[:, cols].astype(jnp.bfloat16)
                mix_buf[half, at, :] = mixed[:, cols].astype(jnp.bfloat16)
            return carry

        lax.fori_loop(0, z_size, down_tile, 0)
        copy = pltpu.make_async_copy(mix_buf, mix_hbm.at[index], mix_sem.at[index])
        copy.start()
        mix_copies.append(copy)
        if index:
            rs_y(index).start()
        turn(n2.at[index], n2_t, index)
        turn(dy, dy_t, index)
        if index + 1 < z_size:
            dy_loads[index + 1].start()

    def rs_y(index):
        return Halves(
            gn_part.at[index, 1 - me_y], gn_y.at[index], rs_y_send.at[index], rs_y_recv.at[index], to_y
        )

    def rs_z(index):
        return Halves(
            gn_s.at[index - 1],
            gn_z.at[index - 1],
            rs_z_send.at[index],
            rs_z_recv.at[index - 1],
            to_z(1),
        )

    def rs_step(index):
        rs_y(index).wait_recv()
        slot = (index - 2) % z_size
        if index != 1:
            Halves(
                gn_s.at[slot], gn_z.at[slot], rs_z_send.at[1], rs_z_recv.at[slot], to_z(1)
            ).wait_recv()

        def add_tile(tile, carry):
            at = pl.ds(pl.multiple_of(tile * TILE, TILE), TILE)
            total = gn_part[index, me_y, at, :].astype(jnp.float32) + gn_y[index, at, :].astype(
                jnp.float32
            )
            if index != 1:
                total = total + gn_z[slot, at, :].astype(jnp.float32)
            if index == 0:
                gm_ref[:, at] = total.T
            else:
                gn_s[index - 1, at, :] = total.astype(jnp.bfloat16)
            return carry

        lax.fori_loop(0, width // TILE, add_tile, 0)
        if index != 0:
            rs_z(index).start()


    def grads(step):
        at = pl.ds(pl.multiple_of(ahead(step) * span, 128), span)
        for kind, source in enumerate((n2_t, n2_t, dy_t)):

            def tile_body(tile, carry, kind=kind, source=source):
                cols = pl.ds(pl.multiple_of(tile * WIDE, WIDE), WIDE)
                w3[kind, at, cols] = dot_nn(source[at, :], h3[kind, :, cols]).astype(jnp.bfloat16)
                return carry

            lax.fori_loop(0, units // WIDE, tile_body, 0)
            for far in (1, 0):
                over_c(kind, step, far).start()

    def over_c(kind, step, far):
        x_at = 1 - me_x if far else me_x
        return remote(
            w3.at[kind, row_block(ahead(step), x_at, 1 - me_c)],
            c_in.at[kind, step, far],
            c_send.at[kind, step, far],
            c_recv.at[kind, step, far],
            to_c,
        )

    def over_x(kind):
        return remote(
            w3.at[kind, row_block(ahead(1), 1 - me_x, me_c)],
            x_in.at[kind],
            x_send.at[kind],
            x_recv.at[kind],
            to_x,
        )

    out_copies = []

    def keep(kind, step, far, block):
        copy = pltpu.make_async_copy(
            block, sums_hbm.at[kind, step, far], out_sem.at[kind, step, far]
        )
        copy.start()
        out_copies.append(copy)

    def core_sums(step):
        pairs = [(kind, far) for kind in range(3) for far in (1, 0)]
        if step == 1:
            pairs.sort(key=lambda pair: -pair[1])
        for kind, far in pairs:
            over_c(kind, step, far).wait_recv()
            x_at = 1 - me_x if far else me_x
            block = w3.at[kind, row_block(ahead(step), x_at, me_c)]
            add_rows(block, [c_in.at[kind, step, far]], block, rows)
            if step != 1:
                keep(kind, step, far, block)
            elif far:
                over_x(kind).start()

    def first_sums():
        for kind in range(3):
            over_x(kind).wait_recv()
            block = w3.at[kind, row_block(ahead(1), me_x, me_c)]
            add_rows(block, [x_in.at[kind]], block, rows)
            keep(kind, 1, 0, block)

    own_load.wait()
    w_loads(lambda copy: copy.wait())

    @pl.when(outer)
    def _():
        w3[:, :, main:] = jnp.zeros((3, width, units - main), jnp.bfloat16)

    chunk(0)
    forward(1)
    forward(2)
    ag_y_in(1).wait_recv()
    chunk(1)
    ag_y_in(2).wait_recv()
    ag_last().start()
    chunk(2)
    rs_step(1)
    ag_z_in(3).wait_recv()
    ag_last().wait_recv()
    chunk(3)
    rs_y(0).start()
    rs_step(2)
    grads(1)
    grads(2)
    core_sums(1)
    rs_step(3)
    grads(3)
    core_sums(2)
    grads(0)
    core_sums(3)
    rs_step(0)
    core_sums(0)

    cot_load = pltpu.make_async_copy(
        dy_hbm.at[0, mine], dy.at[pl.ds(0, own)], load_sem.at[z_size + 3]
    )
    cot_load.start()
    cot_load.wait()
    mid_load.wait()

    def mid_rows(index, total):
        at = pl.ds(pl.multiple_of(index * 32, 32), 32)
        grad, gain_sum = norm_back(mid[at, :], gain_ref[1:2, :], gm_ref[at, :])
        grad = grad + dy[at, :].astype(jnp.float32)
        gm_ref[at, :] = grad
        dy[pl.ds(pl.multiple_of(own + index * 32, 32), 32), :] = grad.astype(jnp.bfloat16)
        return total + gain_sum

    gain_sum = lax.fori_loop(0, own // 32, mid_rows, jnp.zeros((1, width), jnp.float32))
    gm_save = pltpu.make_async_copy(dy.at[pl.ds(own, own)], gm_hbm, load_sem.at[z_size + 3])
    gm_save.start()
    for index in range(4):
        gain_part[index : index + 1, :] = jnp.zeros((1, span), jnp.float32)
        gain_part[4 + index : 5 + index, :] = gain_sum[:, index * span : (index + 1) * span]
    first_sums()
    gm_save.wait()

    for copy in mix_copies[3:] + out_copies:
        copy.wait()
    for index in range(z_size):
        if index in (1, 2):
            ag_y(index).wait_send()
        if index == 3:
            ag_last().wait_send()
        rs_y(index).wait_send()
        if index < z_size - 1:
            ag_z(index).wait_send()
        if index:
            rs_z(index).wait_send()
        for kind in range(3):
            over_c(kind, index, 0).wait_send()
            over_c(kind, index, 1).wait_send()
            if index == 1:
                over_x(kind).wait_send()


def ffn_call(gains, normed, grad_all, weights, mid, rows, main):
    z_size = lax.axis_size("z")
    pair, width = normed.shape
    units = weights.shape[2]
    own = pair // 2
    wide = lambda *lead: pltpu.VMEM((*lead, width), jnp.bfloat16)
    tall = lambda *lead: pltpu.VMEM((*lead, width, own), jnp.bfloat16)
    dma = lambda *lead: pltpu.SemaphoreType.DMA(lead)
    vmem = pl.BlockSpec(memory_space=pltpu.VMEM)
    hbm = pl.BlockSpec(memory_space=pl.ANY)
    return pl.pallas_call(
        functools.partial(ffn_kernel, z_size, main),
        out_shape=(
            jax.ShapeDtypeStruct((own, width), jnp.float32),
            jax.ShapeDtypeStruct((8, width // z_size), jnp.float32),
            jax.ShapeDtypeStruct((z_size, 2, width, own), jnp.bfloat16),
            jax.ShapeDtypeStruct((3, z_size, 2, rows, units), jnp.bfloat16),
            jax.ShapeDtypeStruct((own, width), jnp.bfloat16),
        ),
        in_specs=[vmem, hbm, hbm, hbm, hbm],
        out_specs=(vmem, vmem, hbm, hbm, hbm),
        scratch_shapes=[
            wide(z_size, pair),
            wide(pair),
            pltpu.VMEM(weights.shape, jnp.bfloat16),
            pltpu.VMEM((3, z_size * pair, units), jnp.bfloat16),
            pltpu.VMEM((width, z_size * pair), jnp.bfloat16),
            pltpu.VMEM((width, z_size * pair), jnp.bfloat16),
            tall(z_size, 2),
            tall(2),
            tall(z_size),
            tall(z_size - 1),
            tall(z_size - 1),
            pltpu.VMEM((3, z_size, 2, rows, units), jnp.bfloat16),
            pltpu.VMEM((3, rows, units), jnp.bfloat16),
            pltpu.VMEM((own, width), jnp.float32),
            dma(z_size + 5),
            dma(z_size),
            dma(z_size, 2),
            dma(z_size, 2),
            dma(z_size, 2),
            dma(z_size, 2),
            dma(z_size, 2),
            dma(z_size, 2),
            dma(z_size, 2),
            dma(z_size, 2),
            dma(3, z_size, 2),
            dma(3, z_size, 2),
            dma(3),
            dma(3),
            dma(3, z_size, 2),
        ],
        compiler_params=pltpu.CompilerParams(
            collective_id=0, has_side_effects=True, vmem_limit_bytes=VMEM_BYTES
        ),
        cost_estimate=pl.CostEstimate(
            flops=18 * z_size * pair * width * units,
            bytes_accessed=4 * weights.size + 12 * z_size * pair * width,
            transcendentals=z_size * pair * units,
        ),
    )(gains, normed, grad_all, weights, mid)


def spin(values, table):
    first = values[:, : values.shape[1] // 2]
    turned = first * table[0] + pltpu.roll(first, first.shape[1] // 2, 1) * table[1]
    return jnp.concatenate([turned, values[:, values.shape[1] // 2 :]], axis=1)


def spin_back(values, table):
    first = values[:, : values.shape[1] // 2]
    turned = first * table[0] - pltpu.roll(first, first.shape[1] // 2, 1) * table[1]
    return jnp.concatenate([turned, values[:, values.shape[1] // 2 :]], axis=1)


def head_probs(rotated, keys, allowed):
    scores = jnp.where(allowed > 0.5, matmul_nt(rotated, keys), masked_score)
    weights = jnp.exp(scores - jnp.max(scores, axis=-1, keepdims=True))
    return weights / jnp.sum(weights, axis=-1, keepdims=True)


def ragged_split(columns, parts):
    main = columns // parts // 128 * 128
    return main, main + 128


def pre_kernel(
    z_size,
    tok_ref,
    wkv_ref,
    gain_one_ref,
    gain_two_ref,
    cos_ref,
    sin_ref,
    seg_ref,
    cot_hbm,
    wq_hbm,
    wo_hbm,
    wg_hbm,
    wu_hbm,
    wd_hbm,
    n1_ref,
    rot_ref,
    key_ref,
    val_ref,
    att_ref,
    mid_ref,
    n2_ref,
    gain_ref,
    allow_ref,
    kv_out,
    wq_out,
    wo_out,
    w3_out,
    dy_out,
    kv_w,
    q_w,
    o_w,
    tok,
    part,
    part_y,
    query,
    gain_rows,
    y_send,
    y_recv,
    ky_send,
    ky_recv,
    az_send,
    az_recv,
    ax_send,
    ax_recv,
    ac_send,
    ac_recv,
    fz_send,
    fz_recv,
    fx_send,
    fx_recv,
    fc_send,
    fc_recv,
    dz_send,
    dz_recv,
    dy_send,
    dy_recv,
    local_sem,
):
    me_z, me_x = lax.axis_index("z"), lax.axis_index("x")
    me_c, me_y = lax.axis_index("c"), lax.axis_index("mp")
    own, width = tok_ref.shape
    rows = wq_hbm.shape[0]
    half_rows = wkv_ref.shape[0]
    head = key_ref.shape[1]
    main, units = ragged_split(wg_hbm.shape[1], z_size)
    to_y, to_x, to_c = {"mp": 1 - me_y}, {"x": 1 - me_x}, {"c": 1 - me_c}

    def to_z(step):
        return {"z": lax.rem(me_z + step, z_size)}

    def from_z(step):
        return lax.rem(me_z - step + z_size, z_size)

    def row_block(step, x_at, c_at):
        start = ((from_z(step) * 2 + x_at) * 2 + c_at) * rows
        return pl.ds(pl.multiple_of(start, rows), rows)

    mine = pl.ds(pl.multiple_of(me_y * own, own), own)
    theirs = pl.ds(pl.multiple_of((1 - me_y) * own, own), own)
    bufs = (kv_w, q_w, o_w)
    inputs = (None, wq_hbm, wo_hbm)

    locals_ = []

    def local(src, dst):
        copy = pltpu.make_async_copy(src, dst, local_sem.at[len(locals_)])
        copy.start()
        locals_.append(copy)
        return copy

    here = row_block(0, me_x, me_c)
    own_q = local(wq_hbm, q_w.at[here])
    own_o = local(wo_hbm, o_w.at[here])
    ffn_in = (wg_hbm, wu_hbm, wd_hbm)

    def body_of(target):
        return pl.ds(pl.multiple_of(target * main, 128), main), pl.ds(0, main)

    def tail_of(target):
        start = z_size * main + lax.rem(target + 1, 2) * 128
        return pl.ds(pl.multiple_of(start, 128), 128), pl.ds(main, 128)

    def is_inner(at):
        return (at > 0) & (at < z_size - 1)

    own_f = []
    for kind in range(3):
        src, dst = body_of(me_z)
        own_f.append(local(ffn_in[kind].at[:, src], w3_out.at[kind, here, dst]))

    def own_tail(kind):
        src, dst = tail_of(me_z)
        return pltpu.make_async_copy(
            ffn_in[kind].at[:, src], w3_out.at[kind, here, dst], local_sem.at[12 + kind]
        )

    @pl.when(is_inner(me_z))
    def _():
        for kind in range(3):
            own_tail(kind).start()
    own_d = local(cot_hbm, dy_out.at[0, mine])

    kv_own = pl.ds(pl.multiple_of(here.start + me_y * half_rows, half_rows), half_rows)
    gain_rows[...] = jnp.zeros(gain_rows.shape, jnp.float32)
    gain_rows[0:1, :half_rows] = gain_one_ref[...].astype(jnp.float32)
    gain_rows[1:2, :half_rows] = gain_two_ref[...].astype(jnp.float32)
    spread = gain_rows[...].T
    kv_w[kv_own, : 2 * head] = wkv_ref[...]
    kv_w[kv_own, 2 * head :] = spread[:half_rows, :].astype(jnp.bfloat16)

    barrier = pltpu.get_barrier_semaphore()
    peers = [to_y, to_x, to_c] + [to_z(step) for step in range(1, z_size)]
    for where in peers:
        pl.semaphore_signal(barrier, inc=1, device_id=where, device_id_type=MESH_ID)
    pl.semaphore_wait(barrier, len(peers))

    tok_y = remote(tok_ref, tok.at[mine], y_send.at[1], y_recv.at[1], to_y)
    tok_y_in = remote(tok_ref, tok.at[theirs], y_send.at[1], y_recv.at[1], to_y)
    part_out = remote(part.at[theirs], part_y, y_send.at[2], y_recv.at[2], to_y)
    n2_y = remote(n2_ref.at[mine], n2_ref.at[mine], y_send.at[3], y_recv.at[3], to_y)
    n2_y_in = remote(n2_ref.at[theirs], n2_ref.at[theirs], y_send.at[3], y_recv.at[3], to_y)

    def block_of(kind, step, x_at):
        if kind:
            return row_block(step, x_at, me_c)
        return kv_rows(step, x_at, me_y)

    def kv_rows(step, x_at, y_at):
        start = row_block(step, x_at, me_c).start + y_at * half_rows
        return pl.ds(pl.multiple_of(start, half_rows), half_rows)

    def kv_y(step, far):
        x_at = 1 - me_x if far else me_x
        block = kv_w.at[kv_rows(step, x_at, me_y)]
        slot = step + z_size * far
        return remote(block, block, ky_send.at[slot], ky_recv.at[slot], to_y)

    def kv_y_in(step, far):
        x_at = 1 - me_x if far else me_x
        block = kv_w.at[kv_rows(step, x_at, 1 - me_y)]
        slot = step + z_size * far
        return remote(block, block, ky_send.at[slot], ky_recv.at[slot], to_y)

    def source(kind, step):
        if isinstance(step, int) and step == 0 and kind:
            return inputs[kind]
        return bufs[kind].at[block_of(kind, step, me_x)]

    first_z, last_z = (z_size - 1 - me_z) // (z_size - 1), me_z // (z_size - 1)
    inner = first_z + last_z == 0
    order = (0, 1 + 2 * first_z, 3 - first_z - last_z, 2 - first_z + last_z)
    hops = (
        None,
        (lax.rem(me_z + 1, z_size), 2),
        (lax.rem(me_z + z_size - 1, z_size), 2),
        (lax.rem(3 * (me_z + 3), z_size), lax.rem(2 * me_z + 3, z_size)),
    )

    def a_z_own(kind, right):
        return remote(
            source(kind, 0),
            bufs[kind].at[block_of(kind, 0, me_x)],
            az_send.at[kind, right],
            az_recv.at[kind, 1 if right else z_size - 1],
            to_z(1 if right else z_size - 1),
        )

    def a_z_start(kind):
        @pl.when(last_z == 0)
        def _():
            a_z_own(kind, 1).start()

        @pl.when(first_z == 0)
        def _():
            a_z_own(kind, 0).start()

    def a_z(kind, index):
        target, slot = hops[index]
        block = bufs[kind].at[block_of(kind, order[index], me_x)]
        return remote(
            block, block, az_send.at[kind, 1 + index], az_recv.at[kind, slot], {"z": target}
        )

    def a_z_next(kind, index):
        @pl.when(inner)
        def _():
            a_z(kind, index).start()

    def a_z_done(kind):
        @pl.when(last_z == 0)
        def _():
            a_z_own(kind, 1).wait_send()

        @pl.when(first_z == 0)
        def _():
            a_z_own(kind, 0).wait_send()

        @pl.when(inner)
        def _():
            for index in range(1, z_size):
                a_z(kind, index).wait_send()

    def a_z_in(kind, step):
        block = bufs[kind].at[block_of(kind, step, me_x)]
        return remote(block, block, az_send.at[kind, 0], az_recv.at[kind, step], to_z(1))

    def a_x(kind, step):
        return remote(
            source(kind, step),
            bufs[kind].at[block_of(kind, step, me_x)],
            ax_send.at[kind, step],
            ax_recv.at[kind, step],
            to_x,
        )

    def a_x_in(kind, step):
        block = bufs[kind].at[block_of(kind, step, 1 - me_x)]
        return remote(block, block, ax_send.at[kind, step], ax_recv.at[kind, step], to_x)

    def a_c(kind, step, far):
        x_at = 1 - me_x if far else me_x
        block = bufs[kind].at[row_block(step, x_at, me_c)]
        src = source(kind, step) if kind and not far else block
        slot = step + z_size * far
        return remote(src, block, ac_send.at[kind, slot], ac_recv.at[kind, slot], to_c)

    def a_c_in(kind, step, far):
        x_at = 1 - me_x if far else me_x
        block = bufs[kind].at[row_block(step, x_at, 1 - me_c)]
        slot = step + z_size * far
        return remote(block, block, ac_send.at[kind, slot], ac_recv.at[kind, slot], to_c)

    def f_z(kind, step, act):
        target = lax.rem(me_z + step, z_size)

        def piece(index, src, dst):
            return remote(
                ffn_in[kind].at[:, src],
                w3_out.at[kind, here, dst],
                fz_send.at[kind, step, index],
                fz_recv.at[kind, step, index],
                to_z(step),
            )

        act(piece(0, *body_of(target)))

        @pl.when(is_inner(target))
        def _():
            act(piece(1, *tail_of(target)))

    def f_z_wait(kind, step):
        block = row_block(step, me_x, me_c)

        def piece(index, dst):
            part = w3_out.at[kind, block, dst]
            return remote(
                part, part, fz_send.at[kind, step, index], fz_recv.at[kind, step, index], to_z(step)
            )

        piece(0, pl.ds(0, main)).wait_recv()

        @pl.when(inner)
        def _():
            piece(1, pl.ds(main, 128)).wait_recv()

    def f_x(kind, step, x_at, act):
        for case, columns in ((inner, units), (first_z + last_z > 0, main)):

            @pl.when(case)
            def _(columns=columns):
                block = w3_out.at[kind, row_block(step, x_at, me_c), pl.ds(0, columns)]
                act(remote(block, block, fx_send.at[kind, step], fx_recv.at[kind, step], to_x))

    def f_x_start(kind, step):
        f_x(kind, step, me_x, lambda copy: copy.start())

    def f_x_wait(kind, step):
        f_x(kind, step, 1 - me_x, lambda copy: copy.wait_recv())

    def f_x_done(kind, step):
        f_x(kind, step, me_x, lambda copy: copy.wait_send())

    def f_c(kind, step, far):
        block = w3_out.at[kind, row_block(step, 1 - me_x if far else me_x, me_c)]
        slot = step + z_size * far
        return remote(block, block, fc_send.at[kind, slot], fc_recv.at[kind, slot], to_c)

    def f_c_in(kind, step, far):
        block = w3_out.at[kind, row_block(step, 1 - me_x if far else me_x, 1 - me_c)]
        slot = step + z_size * far
        return remote(block, block, fc_send.at[kind, slot], fc_recv.at[kind, slot], to_c)

    def d_source(step):
        return cot_hbm if isinstance(step, int) else dy_out.at[step, mine]

    def d_z_own(right):
        slot = 1 if right else z_size - 1
        return remote(
            cot_hbm, dy_out.at[slot, mine], dz_send.at[right], dz_recv.at[slot], to_z(slot)
        )

    def d_z_start():
        @pl.when(last_z == 0)
        def _():
            d_z_own(1).start()

        @pl.when(first_z == 0)
        def _():
            d_z_own(0).start()

    def d_z(index):
        target, slot = hops[index]
        return remote(
            dy_out.at[order[index], mine],
            dy_out.at[slot, mine],
            dz_send.at[1 + index],
            dz_recv.at[slot],
            {"z": target},
        )

    def d_z_done():
        @pl.when(last_z == 0)
        def _():
            d_z_own(1).wait_send()

        @pl.when(first_z == 0)
        def _():
            d_z_own(0).wait_send()

        @pl.when(inner)
        def _():
            for index in range(1, z_size):
                d_z(index).wait_send()

    def d_z_in(step):
        block = dy_out.at[step, mine]
        return remote(block, block, dz_send.at[0], dz_recv.at[step], to_z(1))

    def d_y(step):
        return remote(
            d_source(step), dy_out.at[step, mine], dy_send.at[step], dy_recv.at[step], to_y
        )

    def d_y_in(step):
        block = dy_out.at[step, theirs]
        return remote(block, block, dy_send.at[step], dy_recv.at[step], to_y)

    for kind in (1, 0, 2):
        a_z_start(kind)
        a_x(kind, 0).start()
    kv_y(0, 0).start()
    tok_y.start()
    for kind in (1, 2):
        a_c(kind, 0, 0).start()

    for at_end, away in ((first_z, 1), (last_z, z_size - 1)):

        @pl.when(at_end > 0)
        def _(away=away):
            for kind in range(3):
                f_z(kind, away, lambda copy: copy.start())

    tok[mine, :] = tok_ref[...]
    seq = 2 * own
    query_at = lax.broadcasted_iota(jnp.int32, (seq, seq), 0)
    key_at = lax.broadcasted_iota(jnp.int32, (seq, seq), 1)
    segment = seg_ref[...].astype(jnp.float32)
    same = jnp.broadcast_to(segment, (8, seq)).T[:, :1] == segment
    allowed = same & (key_at <= query_at) & (query_at - key_at < WINDOW)
    allow_ref[...] = jnp.where(allowed, 1.0, 0.0)
    d_y(0).start()

    def from_x(index):
        step = order[index]
        for kind in (1, 0, 2):
            a_x_in(kind, step).wait_recv()
            if kind:
                a_c(kind, step, 1).start()
            else:
                kv_y(step, 1).start()

    def from_y(index):
        step = order[index]
        for far in range(2):
            kv_y_in(step, far).wait_recv()
            a_c(0, step, far).start()

    for index in range(1, z_size):
        step = order[index]
        for kind in (1, 0, 2):
            a_z_in(kind, step).wait_recv()
            a_z_next(kind, index)
            a_x(kind, step).start()
            if kind:
                a_c(kind, step, 0).start()
            else:
                kv_y(step, 0).start()
        if index == z_size - 2:
            d_z_start()
        if index == z_size - 1:
            for copy in own_f:
                copy.wait()

            @pl.when(inner)
            def _():
                for kind in range(3):
                    own_tail(kind).wait()

            for kind in range(3):
                for away, sent in ((1, first_z), (3, last_z), (2, 0)):

                    @pl.when(sent == 0 if away != 2 else me_z >= 0)
                    def _(kind=kind, away=away):
                        f_z(kind, away, lambda copy: copy.start())

            for kind in range(3):
                f_x_start(kind, 0)
                f_c(kind, 0, 0).start()
        if index >= 2:
            from_x(index - 2)
            from_y(index - 2)
    for index in (z_size - 2, z_size - 1):
        from_x(index)
        from_y(index)

    def hand_on(kind, step):
        f_z_wait(kind, step)
        f_x_start(kind, step)
        f_c(kind, step, 0).start()

    def cross(kind, step):
        f_x_wait(kind, step)
        f_c(kind, step, 1).start()

    def pass_cotangent(step):
        d_z_in(order[step]).wait_recv()

        @pl.when(inner)
        def _():
            d_z(step).start()

        d_y(order[step]).start()

    def pass_if(case, step):
        @pl.when(case)
        def _():
            pass_cotangent(step)

    outer = first_z + last_z > 0
    tok_y_in.wait_recv()
    own_q.wait()
    own_o.wait()
    for kind in (0, 1):
        for step in range(z_size):
            for far in range(2):
                a_c_in(kind, step, far).wait_recv()

    gains = kv_w[:, 2 * head :].astype(jnp.float32).T[:8, :]
    gain_ref[...] = gains

    def norm_rows(index, carry):
        at = pl.ds(pl.multiple_of(index * 32, 32), 32)
        values = tok[at, :].astype(jnp.float32)
        scale = lax.rsqrt(jnp.mean(values * values, axis=-1, keepdims=True) + epsilon)
        n1_ref[at, :] = (values * scale * gain_ref[0:1, :]).astype(jnp.bfloat16)
        return carry

    lax.fori_loop(0, 2 * own // 32, norm_rows, 0)
    hand_on(0, order[1])
    table = (cos_ref[...], sin_ref[...])
    key_ref[...] = spin(dot_nn(n1_ref[...], kv_w[:, :head]), table).astype(jnp.bfloat16)
    val_ref[...] = dot_nn(n1_ref[...], kv_w[:, head : 2 * head]).astype(jnp.bfloat16)
    hand_on(0, order[2])
    head_scale = head ** (-0.5)
    heads = att_ref.shape[1] // head

    half_cols = att_ref.shape[1] // 2
    for index in range(2):
        cols = pl.ds(index * half_cols, half_cols)
        query[:, cols] = dot_nn(n1_ref[...], q_w[:, cols])

    def attend(index):
        cols = pl.ds(index * head, head)
        rotated = (spin(query[:, cols], table) * head_scale).astype(jnp.bfloat16)
        rot_ref[:, cols] = rotated
        probs = head_probs(rotated, key_ref[...], allow_ref[...]).astype(jnp.bfloat16)
        att_ref[:, cols] = dot_nn(probs, val_ref[...]).astype(jnp.bfloat16)

    tasks = [
        lambda: (pass_cotangent(1), pass_if(inner, 2)),
        lambda: hand_on(0, order[3]),
        lambda: (cross(0, 0), hand_on(1, order[1])),
        lambda: cross(1, 0),
        lambda: (cross(2, 0), hand_on(1, order[2])),
    ]
    for index in range(heads):
        attend(index)
        if index < len(tasks):
            tasks[index]()
    for step in range(z_size):
        for far in range(2):
            a_c_in(2, step, far).wait_recv()
    saves = [
        local(kv_w, kv_out),
        local(q_w, wq_out),
        local(o_w, wo_out),
    ]
    span = width // 4

    def project(index, carry):
        cols = pl.ds(pl.multiple_of(index * span, span), span)
        part[:, cols] = matmul_nt(att_ref[...], o_w[cols, :]).astype(jnp.bfloat16)
        return carry

    lax.fori_loop(0, 4, project, 0)
    part_out.start()
    hand_on(1, order[3])
    pass_if(outer, 2)
    pass_if(inner, 3)
    cross(0, order[1])
    hand_on(2, order[1])
    part_out.wait_recv()

    def middle(index, carry):
        at = pl.ds(pl.multiple_of(index * 32, 32), 32)
        there = pl.ds(pl.multiple_of(me_y * own + index * 32, 32), 32)
        values = (
            tok_ref[at, :].astype(jnp.float32)
            + part[there, :].astype(jnp.float32)
            + part_y[at, :].astype(jnp.float32)
        )
        mid_ref[at, :] = values
        scale = lax.rsqrt(jnp.mean(values * values, axis=-1, keepdims=True) + epsilon)
        n2_ref[there, :] = (values * scale * gain_ref[1:2, :]).astype(jnp.bfloat16)
        return carry

    lax.fori_loop(0, own // 32, middle, 0)
    n2_y.start()
    hand_on(2, order[2])
    cross(0, order[2])
    cross(0, order[3])
    hand_on(2, order[3])
    pass_if(outer, 3)
    for kind in (1, 2):
        for index in (1, 2, 3):
            cross(kind, order[index])
    for kind in range(3):
        for step in range(z_size):
            for far in range(2):
                f_c_in(kind, step, far).wait_recv()
    for step in range(z_size):
        d_y_in(step).wait_recv()
    n2_y_in.wait_recv()

    for kind in range(3):
        a_z_done(kind)
    d_z_done()
    tok_y.wait_send()
    part_out.wait_send()
    n2_y.wait_send()
    own_d.wait()
    for copy in saves:
        copy.wait()
    for step in range(z_size):
        d_y(step).wait_send()
        for far in range(2):
            kv_y(step, far).wait_send()
        for kind in range(3):
            if step:
                f_z(kind, step, lambda copy: copy.wait_send())
            a_x(kind, step).wait_send()
            f_x_done(kind, step)
            for far in range(2):
                a_c(kind, step, far).wait_send()
                f_c(kind, step, far).wait_send()


def pre_call(
    tokens, w_kv, gain_one, gain_two, table, segments, cotangent, w_query, w_out, ffn
):
    z_size = lax.axis_size("z")
    own, width = tokens.shape
    seq = 2 * own
    rows, cols = w_query.shape
    head = table[0].shape[1] * 2
    units = ragged_split(ffn[0].shape[1], z_size)[1]
    low = lambda *dims: jax.ShapeDtypeStruct(dims, jnp.bfloat16)
    full = lambda *dims: jax.ShapeDtypeStruct(dims, jnp.float32)
    dma = lambda *lead: pltpu.SemaphoreType.DMA(lead)
    vmem = pl.BlockSpec(memory_space=pltpu.VMEM)
    hbm = pl.BlockSpec(memory_space=pl.ANY)
    wide = lambda *lead: pltpu.VMEM((*lead, width), jnp.bfloat16)
    return pl.pallas_call(
        functools.partial(pre_kernel, z_size),
        out_shape=(
            low(seq, width),
            low(seq, cols),
            low(seq, head),
            low(seq, head),
            low(seq, cols),
            full(own, width),
            low(seq, width),
            full(8, width),
            full(seq, seq),
            low(width, 2 * head + 128),
            low(width, cols),
            low(width, cols),
            low(3, width, units),
            low(z_size, seq, width),
        ),
        in_specs=[vmem] * 7 + [hbm] * 6,
        out_specs=(vmem,) * 9 + (hbm,) * 5,
        scratch_shapes=[
            pltpu.VMEM((width, 2 * head + 128), jnp.bfloat16),
            pltpu.VMEM((width, cols), jnp.bfloat16),
            pltpu.VMEM((width, cols), jnp.bfloat16),
            wide(seq),
            wide(seq),
            wide(own),
            pltpu.VMEM((seq, cols), jnp.float32),
            pltpu.VMEM((128, 128), jnp.float32),
            dma(4),
            dma(4),
            dma(2 * z_size),
            dma(2 * z_size),
            dma(3, z_size + 1),
            dma(3, z_size),
            dma(3, z_size),
            dma(3, z_size),
            dma(3, 2 * z_size),
            dma(3, 2 * z_size),
            dma(3, z_size, 2),
            dma(3, z_size, 2),
            dma(3, z_size),
            dma(3, z_size),
            dma(3, 2 * z_size),
            dma(3, 2 * z_size),
            dma(z_size + 1),
            dma(z_size),
            dma(z_size),
            dma(z_size),
            dma(16),
        ],
        compiler_params=pltpu.CompilerParams(
            collective_id=1, has_side_effects=True, vmem_limit_bytes=VMEM_BYTES
        ),
        cost_estimate=pl.CostEstimate(
            flops=8 * seq * width * cols,
            bytes_accessed=8 * width * (cols + units),
            transcendentals=seq * seq * cols // head,
        ),
    )(tokens, w_kv, gain_one, gain_two, *table, segments, cotangent, w_query, w_out, *ffn)


def post_kernel(
    z_size,
    main,
    tok_ref,
    gain_ref,
    gain_part_ref,
    n1_ref,
    rot_ref,
    key_ref,
    val_ref,
    att_ref,
    cos_ref,
    sin_ref,
    allow_ref,
    kv_hbm,
    wq_hbm,
    wo_hbm,
    mix_hbm,
    gmf_hbm,
    gmb_hbm,
    mid_hbm,
    sums_hbm,
    mixed_ref,
    tgrad_ref,
    gsum_ref,
    kvg_ref,
    qg_ref,
    og_ref,
    ffn_out,
    kv_w,
    q_w,
    o_w,
    o_part,
    gm,
    gm_f,
    gq,
    gkv,
    kv_sum,
    back_y,
    mix_y,
    mix_z,
    mix_s,
    o_c,
    o_x,
    o_z,
    q_c,
    q_x,
    q_z,
    kv_y,
    kv_c,
    kv_x,
    kv_z,
    gain_own,
    gain_in,
    ffn_in,
    ffn_own,
    load_sem,
    own_sem,
    fx_send,
    fx_recv,
    fz_send,
    fz_recv,
    y_send,
    y_recv,
    my_send,
    my_recv,
    mz_send,
    mz_recv,
    wc_send,
    wc_recv,
    wx_send,
    wx_recv,
    wz_send,
    wz_recv,
    kc_send,
    kc_recv,
    kz_send,
    kz_recv,
    g_send,
    g_recv,
):
    me_z, me_x = lax.axis_index("z"), lax.axis_index("x")
    me_c, me_y = lax.axis_index("c"), lax.axis_index("mp")
    own, width = tok_ref.shape
    seq = 2 * own
    head = key_ref.shape[1]
    cols_here = att_ref.shape[1]
    heads = cols_here // head
    rows = qg_ref.shape[0]
    span = width // z_size
    mine = pl.ds(pl.multiple_of(me_y * own, own), own)
    theirs = pl.ds(pl.multiple_of((1 - me_y) * own, own), own)
    to_y, to_x, to_c = {"mp": 1 - me_y}, {"x": 1 - me_x}, {"c": 1 - me_c}
    head_scale = head ** (-0.5)

    def behind(step):
        return lax.rem(me_z - step + z_size, z_size)

    def to_z(step):
        return {"z": lax.rem(me_z + step, z_size)}

    def row_block(step, x_at, c_at):
        start = ((behind(step) * 2 + x_at) * 2 + c_at) * rows
        return pl.ds(pl.multiple_of(start, rows), rows)

    loads = [
        pltpu.make_async_copy(wo_hbm, o_w, load_sem.at[0]),
        pltpu.make_async_copy(wq_hbm, q_w, load_sem.at[1]),
        pltpu.make_async_copy(
            kv_hbm.at[:, :, :, :, :, pl.ds(0, 2 * head)], kv_w, load_sem.at[2]
        ),
    ]
    for step in range(z_size):
        loads.append(
            pltpu.make_async_copy(mix_hbm.at[step, me_y], mix_s.at[step], load_sem.at[3 + step])
        )
    loads.append(pltpu.make_async_copy(gmf_hbm, gm_f, load_sem.at[3 + z_size]))
    loads.append(pltpu.make_async_copy(gmb_hbm, gm.at[mine], load_sem.at[4 + z_size]))
    mid_load = pltpu.make_async_copy(mid_hbm, gm_f, load_sem.at[5 + z_size])
    for load in loads:
        load.start()

    barrier = pltpu.get_barrier_semaphore()
    peers = [to_y, to_x, to_c] + [to_z(step) for step in range(1, z_size)]
    for where in peers:
        pl.semaphore_signal(barrier, inc=1, device_id=where, device_id_type=MESH_ID)
    pl.semaphore_wait(barrier, len(peers))

    tasks = [(step, kind) for step in (2, 3) for kind in range(3)]

    def f_x(index):
        step, kind = tasks[index]
        return remote(
            sums_hbm.at[kind, step, 1],
            ffn_in.at[index],
            fx_send.at[index],
            fx_recv.at[index],
            to_x,
        )

    def f_own(index):
        step, kind = tasks[index]
        return pltpu.make_async_copy(
            sums_hbm.at[kind, step, 0], ffn_own.at[index % 2], own_sem.at[index % 2]
        )

    def f_z(step, kind, source_z, act):
        for case, columns in (
            ((source_z > 0) & (source_z < z_size - 1), ffn_out.shape[3]),
            ((source_z == 0) | (source_z == z_size - 1), main),
        ):

            @pl.when(case)
            def _(columns=columns):
                cols = pl.ds(0, columns)
                if step == 1:
                    src = sums_hbm.at[kind, 1, 0, :, cols]
                else:
                    src = ffn_in.at[tasks.index((step, kind)), :, cols]
                act(
                    remote(
                        src,
                        ffn_out.at[kind, step, :, cols],
                        fz_send.at[kind, step],
                        fz_recv.at[kind, step],
                        to_z(step),
                    )
                )

    def tick(index):
        step, kind = tasks[index]
        f_x(index).wait_recv()
        f_own(index).wait()
        block = ffn_in.at[index]
        add_rows(block, [ffn_own.at[index % 2]], block, rows)
        if index + 2 < len(tasks):
            f_own(index + 2).start()
        f_z(step, kind, me_z, lambda copy: copy.start())

    def f_x_own(kind):
        return remote(
            sums_hbm.at[kind, 0, 1],
            ffn_out.at[kind, 0],
            fx_send.at[len(tasks) + kind],
            fx_recv.at[len(tasks) + kind],
            to_x,
        )

    f_own(0).start()
    f_own(1).start()
    for index in range(len(tasks)):
        f_x(index).start()
    for kind in range(3):
        f_z(1, kind, me_z, lambda copy: copy.start())

    gm_y = remote(gmb_hbm, gm.at[mine], y_send.at[0], y_recv.at[0], to_y)
    gm_y_in = remote(gm.at[theirs], gm.at[theirs], y_send.at[0], y_recv.at[0], to_y)
    gm_y.start()

    first_z, last_z = (z_size - 1 - me_z) // (z_size - 1), me_z // (z_size - 1)
    inner = first_z + last_z == 0
    order = (
        0,
        1 + (me_z + 1) // 2,
        2 + (2 * me_z - 3) * (1 - first_z - last_z),
        3 - 2 * (me_z // 2),
    )
    right = (None, 1 - me_z // 2, (3 - me_z) * (2 - me_z) // 6 + me_z // 2 * (1 - last_z), 1 - me_z // 2)

    def hop_slot(index):
        step, way = order[index], right[index]
        return way * lax.rem(step + 1, z_size) + (1 - way) * (step - 1 + 4 * ((3 - step) // 2))

    def hop_target(index):
        return {"z": me_z + 2 * right[index] - 1}

    def mix_over_y(step):
        return remote(
            mix_hbm.at[step, 1 - me_y], mix_y.at[step], my_send.at[step], my_recv.at[step], to_y
        )

    def mix_over_z(index):
        slot = hop_slot(index)
        return remote(
            mix_s.at[order[index]],
            mix_z.at[slot],
            mz_send.at[index],
            mz_recv.at[slot],
            hop_target(index),
        )

    def mix_z_in(slot):
        return remote(mix_z.at[slot], mix_z.at[slot], mz_send.at[1], mz_recv.at[slot], to_z(1))

    def mix_add(step, others, last):
        def add_tile(tile, carry):
            at = pl.ds(pl.multiple_of(tile * TILE, TILE), TILE)
            total = mix_s[step, at, :].astype(jnp.float32)
            for other in others:
                total = total + other[at, :].astype(jnp.float32)
            if last:
                mixed_ref[:, at] = (gm_f[:, at] + total.T).astype(jnp.bfloat16)
            else:
                mix_s[step, at, :] = total.astype(jnp.bfloat16)
            return carry

        lax.fori_loop(0, width // TILE, add_tile, 0)

    def mix_step(index):
        step = order[index]
        mix_over_y(step).wait_recv()
        from_y = mix_y.at[step]
        if index:

            @pl.when(inner)
            def _():
                mix_z_in(step).wait_recv()
                mix_add(step, [from_y, mix_z.at[step]], False)

            @pl.when(first_z + last_z > 0)
            def _():
                mix_add(step, [from_y], False)

            mix_over_z(index).start()
        else:
            mid_load.wait()

            @pl.when(first_z == 0)
            def _():
                mix_z_in(0).wait_recv()

            @pl.when(last_z == 0)
            def _():
                mix_z_in(z_size).wait_recv()

            @pl.when(inner)
            def _():
                mix_add(0, [from_y, mix_z.at[0], mix_z.at[z_size]], True)

            @pl.when(first_z > 0)
            def _():
                mix_add(0, [from_y, mix_z.at[z_size]], True)

            @pl.when(last_z > 0)
            def _():
                mix_add(0, [from_y, mix_z.at[0]], True)

    for index in (1, 2, 3, 0):
        mix_over_y(order[index]).start()

    kinds = ((o_part, o_c, o_x, o_z, og_ref), (o_w, q_c, q_x, q_z, qg_ref))

    def w_c(kind, step, far):
        x_at = 1 - me_x if far else me_x
        return remote(
            kinds[kind][0].at[row_block(step, x_at, 1 - me_c)],
            kinds[kind][1].at[step, far],
            wc_send.at[kind, step, far],
            wc_recv.at[kind, step, far],
            to_c,
        )

    def w_x(kind, step):
        return remote(
            kinds[kind][0].at[row_block(step, 1 - me_x, me_c)],
            kinds[kind][2].at[step],
            wx_send.at[kind, step],
            wx_recv.at[kind, step],
            to_x,
        )

    def w_z(kind, index):
        step, slot = order[index], hop_slot(index)
        return remote(
            kinds[kind][0].at[row_block(step, me_x, me_c)],
            kinds[kind][3].at[slot],
            wz_send.at[kind, index],
            wz_recv.at[kind, slot],
            hop_target(index),
        )

    def w_z_in(kind, slot):
        block = kinds[kind][3].at[slot]
        return remote(block, block, wz_send.at[kind, 1], wz_recv.at[kind, slot], to_z(1))

    def w_x_stage(kind, index):
        step = order[index]
        w_c(kind, step, 1).wait_recv()
        block = kinds[kind][0].at[row_block(step, 1 - me_x, me_c)]
        add_rows(block, [kinds[kind][1].at[step, 1]], block, rows)
        w_x(kind, step).start()

    def w_z_stage(kind, index):
        part, from_c, from_x, from_z, result = kinds[kind]
        step = order[index]
        w_c(kind, step, 0).wait_recv()
        w_x(kind, step).wait_recv()
        block = part.at[row_block(step, me_x, me_c)]
        others = [from_c.at[step, 0], from_x.at[step]]
        if index:

            @pl.when(inner)
            def _():
                w_z_in(kind, step).wait_recv()
                add_rows(block, [*others, from_z.at[step]], block, rows)

            @pl.when(first_z + last_z > 0)
            def _():
                add_rows(block, others, block, rows)

            w_z(kind, index).start()
        else:

            @pl.when(first_z == 0)
            def _():
                w_z_in(kind, 0).wait_recv()

            @pl.when(last_z == 0)
            def _():
                w_z_in(kind, z_size).wait_recv()

            @pl.when(inner)
            def _():
                add_rows(block, [*others, from_z.at[0], from_z.at[z_size]], result, rows)

            @pl.when(first_z > 0)
            def _():
                add_rows(block, [*others, from_z.at[z_size]], result, rows)

            @pl.when(last_z > 0)
            def _():
                add_rows(block, [*others, from_z.at[0]], result, rows)

    def w_product(kind, index, left, values):
        step = order[index]
        at = pl.ds(pl.multiple_of(behind(step) * span, 128), span)
        turned = left[:, at].T

        def tile_body(tile, carry):
            cols = pl.ds(pl.multiple_of(tile * TILE, TILE), TILE)
            kinds[kind][0][at, cols] = dot_nn(turned, values[:, cols]).astype(jnp.bfloat16)
            return carry

        lax.fori_loop(0, cols_here // TILE, tile_body, 0)
        for far in (1, 0):
            w_c(kind, step, far).start()

    tick(0)
    tick(1)
    loads[-1].wait()
    gm_y_in.wait_recv()
    w_product(0, 1, gm, att_ref)
    w_product(0, 2, gm, att_ref)
    w_x_stage(0, 1)
    w_product(0, 3, gm, att_ref)
    w_x_stage(0, 2)
    tick(2)
    w_product(0, 0, gm, att_ref)
    w_x_stage(0, 3)
    for load in loads[:-1]:
        load.wait()

    kv_sum[...] = jnp.zeros(kv_sum.shape, jnp.float32)
    table = (cos_ref[...], sin_ref[...])

    for index in range(2):
        cols = pl.ds(index * (cols_here // 2), cols_here // 2)
        gq[:, cols] = dot_nn(gm[...], o_w[:, cols]).astype(jnp.bfloat16)

    def attend_back(index):
        cols = pl.ds(index * head, head)
        grad_vals = gq[:, cols]
        rotated = rot_ref[:, cols]
        probs = head_probs(rotated, key_ref[...], allow_ref[...])
        grad_probs = matmul_nt(grad_vals, val_ref[...])
        delta = jnp.sum(probs * grad_probs, axis=-1, keepdims=True)
        grad_scores = (probs * (grad_probs - delta)).astype(jnp.bfloat16)
        grad_rot = dot_nn(grad_scores, key_ref[...])
        gq[:, cols] = (spin_back(grad_rot, table) * head_scale).astype(jnp.bfloat16)
        kv_sum[0] += matmul_tn(grad_scores, rotated)
        kv_sum[1] += matmul_tn(probs.astype(jnp.bfloat16), grad_vals)

    for index in range(heads):
        attend_back(index)
        if index == 0:
            w_x_stage(0, 0)
        if 3 + index < len(tasks):
            tick(3 + index)
        if index == heads - 1:
            mix_step(1)
    gkv[:, :head] = spin_back(kv_sum[0], table).astype(jnp.bfloat16)
    gkv[:, head:] = kv_sum[1].astype(jnp.bfloat16)

    w_product(1, 1, n1_ref, gq)
    w_product(1, 2, n1_ref, gq)
    w_x_stage(1, 1)
    w_z_stage(0, 1)
    w_product(1, 3, n1_ref, gq)
    w_x_stage(1, 2)
    w_product(1, 0, n1_ref, gq)
    w_x_stage(1, 3)
    w_x_stage(1, 0)
    for kind in range(3):
        f_x_own(kind).start()

    gm_y.wait_send()
    back = gm
    def input_tile(index, carry):
        at = pl.ds(pl.multiple_of(index * span, 128), span)
        back[:, at] = (
            matmul_nt(gq[...], q_w[at, :]) + matmul_nt(gkv[...], kv_w[index].reshape(span, 2 * head))
        ).astype(jnp.bfloat16)
        return carry

    lax.fori_loop(0, z_size, input_tile, 0)
    back_out = remote(back.at[theirs], back_y, y_send.at[1], y_recv.at[1], to_y)
    back_out.start()

    kv_part = kv_w

    def kv_tile(index, carry):
        at = pl.ds(pl.multiple_of(index * span, 128), span)
        product = dot_nn(n1_ref[:, at].T, gkv[...]).astype(jnp.bfloat16)
        kv_part[index] = product.reshape(kv_part.shape[1:])
        return carry

    lax.fori_loop(0, z_size, kv_tile, 0)
    kv_over_y = remote(kv_part.at[:, :, :, 1 - me_y], kv_y, y_send.at[2], y_recv.at[2], to_y)
    kv_over_y.start()
    mix_step(2)
    w_z_stage(0, 2)
    mix_step(3)
    w_z_stage(0, 3)

    back_out.wait_recv()

    def input_rows(index, total):
        at = pl.ds(pl.multiple_of(index * 32, 32), 32)
        there = pl.ds(pl.multiple_of(me_y * own + index * 32, 32), 32)
        upstream = back[there, :].astype(jnp.float32) + back_y[at, :].astype(jnp.float32)
        grad, gain_part = norm_back(
            tok_ref[at, :].astype(jnp.float32), gain_ref[0:1, :], upstream
        )
        tgrad_ref[at, :] = (gm_f[at, :] + grad).astype(jnp.bfloat16)
        return total + gain_part

    attn_gain_part = lax.fori_loop(
        0, own // 32, input_rows, jnp.zeros((1, width), jnp.float32)
    )
    for index in range(4):
        at = slice(index * span, (index + 1) * span)
        gain_own[0, index : index + 1, :] = attn_gain_part[:, at]
        gain_own[0, 4 + index : 5 + index, :] = gain_part_ref[4 + index : 5 + index, :]

    def gain_send(stage, where):
        return remote(
            gain_own.at[stage], gain_in.at[stage], g_send.at[stage], g_recv.at[stage], where
        )

    gain_hops = [gain_send(0, to_y), gain_send(1, to_c), gain_send(2, to_x)]
    gain_last = [
        remote(
            gain_own.at[3], gain_in.at[2 + step], g_send.at[2 + step], g_recv.at[2 + step], to_z(step)
        )
        for step in range(1, z_size)
    ]

    def gain_fold(stage):
        gain_hops[stage].wait_recv()
        gain_own[stage + 1] = gain_own[stage] + gain_in[stage]

    gain_hops[0].start()
    mid_load.start()
    w_z_stage(1, 1)
    w_z_stage(0, 0)
    w_z_stage(1, 2)
    gain_fold(0)
    gain_hops[1].start()
    mix_step(0)
    w_z_stage(1, 3)
    gain_fold(1)
    gain_hops[2].start()
    kv_over_y.wait_recv()

    def kv_add_y(index, carry):
        for x_at in range(2):
            for c_at in range(2):
                block = kv_part.at[index, x_at, c_at, me_y]
                block[...] = (
                    block[...].astype(jnp.float32) + kv_y[index, x_at, c_at].astype(jnp.float32)
                ).astype(jnp.bfloat16)
        return carry

    lax.fori_loop(0, z_size, kv_add_y, 0)
    kv_over_c = remote(
        kv_part.at[:, :, 1 - me_c, me_y], kv_c, kc_send.at[0], kc_recv.at[0], to_c
    )
    kv_over_c.start()
    gain_fold(2)
    for copy in gain_last:
        copy.start()
    kv_over_c.wait_recv()

    def kv_add_c(index, carry):
        for x_at in range(2):
            block = kv_part.at[index, x_at, me_c, me_y]
            block[...] = (
                block[...].astype(jnp.float32) + kv_c[index, x_at].astype(jnp.float32)
            ).astype(jnp.bfloat16)
        return carry

    lax.fori_loop(0, z_size, kv_add_c, 0)
    kv_over_x = remote(
        kv_part.at[:, 1 - me_x, me_c, me_y], kv_x, kc_send.at[1], kc_recv.at[1], to_x
    )
    kv_over_x.start()
    w_z_stage(1, 0)
    kv_over_x.wait_recv()

    def kv_add_x(index, carry):
        block = kv_part.at[index, me_x, me_c, me_y]
        block[...] = (
            block[...].astype(jnp.float32) + kv_x[index].astype(jnp.float32)
        ).astype(jnp.bfloat16)
        return carry

    lax.fori_loop(0, z_size, kv_add_x, 0)
    kv_over_z = [
        remote(
            kv_part.at[lax.rem(me_z + step, z_size), me_x, me_c, me_y],
            kv_z.at[step - 1],
            kz_send.at[step],
            kz_recv.at[step],
            to_z(step),
        )
        for step in range(1, z_size)
    ]
    for copy in kv_over_z:
        copy.start()
    for copy in gain_last:
        copy.wait_recv()
    gsum_ref[...] = gain_own[3] + gain_in[3] + gain_in[4] + gain_in[5]
    for copy in kv_over_z:
        copy.wait_recv()
    kvg_ref[...] = (
        kv_part[me_z, me_x, me_c, me_y].astype(jnp.float32)
        + kv_z[0].astype(jnp.float32)
        + kv_z[1].astype(jnp.float32)
        + kv_z[2].astype(jnp.float32)
    )

    back_out.wait_send()
    kv_over_y.wait_send()
    kv_over_c.wait_send()
    kv_over_x.wait_send()
    for kind in range(3):
        f_x_own(kind).wait()
    for index in range(len(tasks)):
        f_x(index).wait_send()
    for step in range(1, z_size):
        for kind in range(3):
            f_z(step, kind, me_z, lambda copy: copy.wait_send())
            f_z(step, kind, behind(step), lambda copy: copy.wait_recv())
    for copy in gain_hops + gain_last + kv_over_z:
        copy.wait_send()
    for step in range(z_size):
        mix_over_y(step).wait_send()
        if step:
            mix_over_z(step).wait_send()
        for kind in range(2):
            w_c(kind, step, 0).wait_send()
            w_c(kind, step, 1).wait_send()
            w_x(kind, step).wait_send()
            if step:
                w_z(kind, step).wait_send()


def post_call(
    tokens,
    gains,
    gain_part,
    normed_one,
    rotated,
    keys,
    values,
    attn_vals,
    table,
    allowed,
    kv_weight,
    query_weight,
    out_weight,
    mix_parts,
    grad_mid,
    grad_mid_low,
    mid,
    ffn_sums,
    main,
):
    z_size = lax.axis_size("z")
    own, width = tokens.shape
    seq = 2 * own
    head = keys.shape[1]
    cols = attn_vals.shape[1]
    rows = width // (4 * z_size)
    units = ffn_sums.shape[4]
    low = lambda *dims: pltpu.VMEM(dims, jnp.bfloat16)
    full = lambda *dims: pltpu.VMEM(dims, jnp.float32)
    out_full = lambda *dims: jax.ShapeDtypeStruct(dims, jnp.float32)
    out_low = lambda *dims: jax.ShapeDtypeStruct(dims, jnp.bfloat16)
    dma = lambda *lead: pltpu.SemaphoreType.DMA(lead)
    vmem = pl.BlockSpec(memory_space=pltpu.VMEM)
    hbm = pl.BlockSpec(memory_space=pl.ANY)
    z = z_size
    return pl.pallas_call(
        functools.partial(post_kernel, z_size, main),
        out_shape=(
            out_low(own, width),
            out_low(own, width),
            out_full(8, width // z),
            out_full(rows // 2, 2 * head),
            out_full(rows, cols),
            out_full(rows, cols),
            out_low(3, z, rows, units),
        ),
        in_specs=[vmem] * 11 + [hbm] * 8,
        out_specs=(vmem,) * 6 + (hbm,),
        scratch_shapes=[
            low(z, 2, 2, 2, rows // 2, 2 * head),
            low(width, cols),
            low(width, cols),
            low(width, cols),
            low(seq, width),
            full(own, width),
            low(seq, cols),
            low(seq, 2 * head),
            full(2, seq, head),
            low(own, width),
            low(z, width, own),
            low(z + 1, width, own),
            low(z, width, own),
            low(z, 2, rows, cols),
            low(z, rows, cols),
            low(z + 1, rows, cols),
            low(z, 2, rows, cols),
            low(z, rows, cols),
            low(z + 1, rows, cols),
            low(z, 2, 2, rows // 2, 2 * head),
            low(z, 2, rows // 2, 2 * head),
            low(z, rows // 2, 2 * head),
            low(z - 1, rows // 2, 2 * head),
            full(4, 8, width // z),
            full(6, 8, width // z),
            low(6, rows, units),
            low(2, rows, units),
            dma(6 + z),
            dma(2),
            dma(9),
            dma(9),
            dma(3, z),
            dma(3, z),
            dma(3),
            dma(3),
            dma(z),
            dma(z),
            dma(z),
            dma(z + 1),
            dma(2, z, 2),
            dma(2, z, 2),
            dma(2, z),
            dma(2, z),
            dma(2, z),
            dma(2, z + 1),
            dma(2),
            dma(2),
            dma(z),
            dma(z),
            dma(6),
            dma(6),
        ],
        compiler_params=pltpu.CompilerParams(
            collective_id=2, has_side_effects=True, vmem_limit_bytes=VMEM_BYTES
        ),
        cost_estimate=pl.CostEstimate(
            flops=14 * seq * width * cols,
            bytes_accessed=10 * width * cols,
            transcendentals=seq * seq * cols // head,
        ),
    )(
        tokens,
        gains,
        gain_part,
        normed_one,
        rotated,
        keys,
        values,
        attn_vals,
        *table,
        allowed,
        kv_weight.reshape(z, 2, 2, 2, rows // 2, kv_weight.shape[1]),
        query_weight,
        out_weight,
        mix_parts,
        grad_mid,
        grad_mid_low,
        mid,
        ffn_sums,
    )


def layout_kernel(
    z_size,
    main,
    sum_ref,
    ffn_ref,
    q_ref,
    o_ref,
    kv_ref,
    mixed_in,
    tgrad_in,
    wg_ref,
    wu_ref,
    wd_ref,
    qg_ref,
    og_ref,
    kvg_ref,
    mixed_ref,
    tgrad_ref,
):
    me_z = lax.axis_index("z")
    for kind, out in enumerate((wg_ref, wu_ref, wd_ref)):
        for step in range(z_size):
            at = lax.rem(me_z - step + z_size, z_size)
            values = ffn_ref[kind, step].astype(jnp.float32)
            if step == 0:
                values = values + sum_ref[kind, 0, 0].astype(jnp.float32)
            body = pl.ds(pl.multiple_of(at * main, 128), main)
            out[:, body] = values[:, :main]

            @pl.when((at > 0) & (at < z_size - 1))
            def _(out=out, at=at, values=values):
                tail = z_size * main + lax.rem(at + 1, 2) * 128
                out[:, pl.ds(pl.multiple_of(tail, 128), 128)] = values[:, main:]
    qg_ref[...] = q_ref[...]
    og_ref[...] = o_ref[...]
    kvg_ref[...] = kv_ref[...]
    mixed_ref[...] = mixed_in[...]
    tgrad_ref[...] = tgrad_in[...]


def layout_call(ffn_sums, ffn_grads, query_grad, out_grad, kv_grad, mixed, tokens_grad, ffn_cols):
    z_size = lax.axis_size("z")
    main, units = ragged_split(ffn_cols, z_size)
    rows, cols = query_grad.shape
    parts = rows // 32
    kv_rows = kv_grad.shape[0] // parts
    full = lambda *dims: jax.ShapeDtypeStruct(dims, jnp.float32)
    row = lambda height, width: pl.BlockSpec((height, width), lambda index: (index, 0))
    own, width = mixed.shape
    share = pl.BlockSpec((own, width // parts), lambda index: (0, index))
    specs = [row(32, cols), row(32, cols), row(kv_rows, kv_grad.shape[1]), share, share]
    return pl.pallas_call(
        functools.partial(layout_kernel, z_size, main),
        grid=(parts,),
        out_shape=(
            *[full(rows, ffn_cols)] * 3,
            full(rows, cols),
            full(rows, cols),
            full(*kv_grad.shape),
            jax.ShapeDtypeStruct(mixed.shape, jnp.bfloat16),
            jax.ShapeDtypeStruct(mixed.shape, jnp.bfloat16),
        ),
        in_specs=[
            pl.BlockSpec((3, 1, 1, 32, units), lambda index: (0, 0, 0, index, 0)),
            pl.BlockSpec((3, z_size, 32, units), lambda index: (0, 0, index, 0)),
            *specs,
        ],
        out_specs=(*[row(32, ffn_cols)] * 3, *specs),
        compiler_params=pltpu.CompilerParams(vmem_limit_bytes=VMEM_BYTES),
    )(ffn_sums, ffn_grads, query_grad, out_grad, kv_grad, mixed, tokens_grad)


FF_SPLIT = 4


def ffn_pass(normed, grad_out, gate_weight, up_weight, down_weight):
    gate = jnp.dot(normed, gate_weight, preferred_element_type=jnp.float32)
    up_proj = jnp.dot(normed, up_weight, preferred_element_type=jnp.float32)
    grad_hidden = jnp.dot(grad_out, down_weight, preferred_element_type=jnp.float32)
    product, pull = jax.vjp(gelu_product, gate, up_proj)
    hidden = product.astype(jnp.bfloat16)
    grad_gate_f, grad_up_f = pull(grad_hidden)
    grad_gate = grad_gate_f.astype(jnp.bfloat16)
    grad_up = grad_up_f.astype(jnp.bfloat16)
    mixed_part = matmul_nt(hidden, down_weight).astype(jnp.bfloat16)
    normed_part = (matmul_nt(grad_gate, gate_weight) + matmul_nt(grad_up, up_weight)).astype(
        jnp.bfloat16
    )
    weight_parts = [
        matmul_tn(normed, grad_gate).astype(jnp.bfloat16),
        matmul_tn(normed, grad_up).astype(jnp.bfloat16),
        matmul_tn(grad_out, hidden).astype(jnp.bfloat16),
    ]
    return mixed_part, normed_part, weight_parts


def shards_general(
    tokens,
    segments,
    positions,
    cotangent,
    attn_gain,
    ffn_gain,
    w_kv,
    w_query,
    w_out,
    w_gate,
    w_up,
    w_down,
):
    everywhere = ("z", "xc", "mp")
    dp = ("z", "xc")
    z_size = lax.axis_size("z")
    xc_size = lax.axis_size("xc")
    gains = lax.all_gather(
        jnp.stack([attn_gain, ffn_gain], axis=1), everywhere, axis=0, tiled=True
    ).astype(jnp.float32)
    gain_one, gain_two = gains[:, 0], gains[:, 1]
    kv_weight = lax.all_gather(w_kv, everywhere, axis=0, tiled=True)
    head_dim = kv_weight.shape[1] // 2
    width = tokens.shape[1]
    seq_len = segments.shape[0]
    heads_here = w_query.shape[1] // head_dim
    scale = head_dim ** (-0.5)
    cosine, sine = rotary_angles(positions, head_dim)
    inputs_f = tokens.astype(jnp.float32)
    tokens_all = lax.all_gather(tokens, "mp", axis=0, tiled=True)
    normed_one = norm_gain(tokens_all.astype(jnp.float32), gain_one).astype(jnp.bfloat16)
    query_weight = lax.all_gather(w_query, dp, axis=0, tiled=True)
    out_weight = lax.all_gather(w_out, dp, axis=0, tiled=True)

    rows = w_gate.shape[0]
    unit = w_gate.shape[1] // z_size

    def spread(weight):
        pieces = weight.reshape(rows, z_size, unit).transpose(1, 0, 2)
        pieces = lax.all_to_all(pieces, "z", split_axis=0, concat_axis=0, tiled=True)
        return lax.all_gather(pieces, "xc", axis=1, tiled=False).reshape(width, unit)

    gate_weight, up_weight, down_weight = spread(w_gate), spread(w_up), spread(w_down)
    grad_all = lax.all_gather(cotangent, ("z", "mp"), axis=0, tiled=True)

    query = jnp.dot(normed_one, query_weight, preferred_element_type=jnp.float32).reshape(
        seq_len, heads_here, head_dim
    )
    rotated = (rotate(query, cosine[:, None], sine[:, None]) * scale).astype(jnp.bfloat16)
    keyval = jnp.dot(normed_one, kv_weight, preferred_element_type=jnp.float32)
    keys = rotate(keyval[:, :head_dim], cosine, sine).astype(jnp.bfloat16)
    values = keyval[:, head_dim:].astype(jnp.bfloat16)
    allowed = block_allowed(segments, 0, seq_len)
    scores = jnp.einsum("thd,sd->hts", rotated, keys, preferred_element_type=jnp.float32)
    scores = jnp.where(allowed[None], scores, masked_score)
    row_max = jnp.max(scores, axis=-1, keepdims=True)
    weights = jnp.exp(scores - row_max)
    probs = weights / jnp.sum(weights, axis=-1, keepdims=True)
    probs_low = probs.astype(jnp.bfloat16)
    attn_vals = (
        jnp.einsum("hts,sd->thd", probs_low, values, preferred_element_type=jnp.float32)
        .reshape(seq_len, heads_here * head_dim)
        .astype(jnp.bfloat16)
    )
    mid = inputs_f + lax.psum_scatter(
        matmul_nt(attn_vals, out_weight).astype(jnp.bfloat16),
        "mp",
        scatter_dimension=0,
        tiled=True,
    ).astype(jnp.float32)
    normed_two = norm_gain(mid, gain_two).astype(jnp.bfloat16)
    normed_all = lax.all_gather(normed_two, ("z", "mp"), axis=0, tiled=True)

    mixed_part, normed_part, weight_parts = ffn_pass(
        normed_all, grad_all, gate_weight, up_weight, down_weight
    )
    grad_normed_two = lax.psum_scatter(
        normed_part, ("z", "mp"), scatter_dimension=0, tiled=True
    ).astype(jnp.float32)
    mixed = (
        mid
        + lax.psum_scatter(mixed_part, ("z", "mp"), scatter_dimension=0, tiled=True).astype(
            jnp.float32
        )
    ).astype(jnp.bfloat16)

    def collect(part):
        pieces = part.reshape(z_size, xc_size, rows, unit).transpose(1, 0, 2, 3)
        pieces = pieces.reshape(xc_size * z_size * rows, unit)
        pieces = lax.psum_scatter(pieces, "xc", scatter_dimension=0, tiled=True)
        pieces = pieces.reshape(z_size, rows, unit)
        pieces = lax.all_to_all(pieces, "z", split_axis=0, concat_axis=0, tiled=True)
        return pieces.transpose(1, 0, 2).reshape(rows, z_size * unit).astype(jnp.float32)

    w_gate_grad, w_up_grad, w_down_grad = [collect(part) for part in weight_parts]

    norm_pull_two = jax.vjp(norm_gain, mid, gain_two)[1]
    grad_mid_norm, grad_gain_two = norm_pull_two(grad_normed_two)
    grad_mid = cotangent.astype(jnp.float32) + grad_mid_norm
    grad_mid_all = lax.all_gather(grad_mid.astype(jnp.bfloat16), "mp", axis=0, tiled=True)
    grad_vals = (
        jnp.dot(grad_mid_all, out_weight, preferred_element_type=jnp.float32)
        .astype(jnp.bfloat16)
        .reshape(seq_len, heads_here, head_dim)
    )
    grad_probs = jnp.einsum("thd,sd->hts", grad_vals, values, preferred_element_type=jnp.float32)
    delta = jnp.sum(probs * grad_probs, axis=-1, keepdims=True)
    grad_scores = (probs * (grad_probs - delta)).astype(jnp.bfloat16)
    grad_rot = jnp.einsum("hts,sd->thd", grad_scores, keys, preferred_element_type=jnp.float32)
    key_sum = jnp.einsum("hts,thd->sd", grad_scores, rotated, preferred_element_type=jnp.float32)
    value_sum = jnp.einsum("hts,thd->sd", probs_low, grad_vals, preferred_element_type=jnp.float32)
    grad_query = (
        (unrotate(grad_rot, cosine[:, None], sine[:, None]) * scale)
        .reshape(seq_len, heads_here * head_dim)
        .astype(jnp.bfloat16)
    )
    grad_kv = jnp.concatenate([unrotate(key_sum, cosine, sine), value_sum], axis=1).astype(
        jnp.bfloat16
    )
    grad_normed_one = lax.psum_scatter(
        (matmul_nt(grad_query, query_weight) + matmul_nt(grad_kv, kv_weight)).astype(jnp.bfloat16),
        "mp",
        scatter_dimension=0,
        tiled=True,
    ).astype(jnp.float32)
    norm_pull_one = jax.vjp(norm_gain, inputs_f, gain_one)[1]
    grad_input_norm, grad_gain_one = norm_pull_one(grad_normed_one)
    tokens_grad = (grad_mid + grad_input_norm).astype(jnp.bfloat16)

    w_query_grad = lax.psum_scatter(
        matmul_tn(normed_one, grad_query).astype(jnp.bfloat16), dp, scatter_dimension=0, tiled=True
    ).astype(jnp.float32)
    w_out_grad = lax.psum_scatter(
        matmul_tn(grad_mid_all, attn_vals).astype(jnp.bfloat16), dp, scatter_dimension=0, tiled=True
    ).astype(jnp.float32)
    small = jnp.concatenate(
        [matmul_tn(normed_one, grad_kv), grad_gain_one[:, None], grad_gain_two[:, None]], axis=1
    )
    small = lax.psum_scatter(small, everywhere, scatter_dimension=0, tiled=True)
    kv_grad = small[:, : 2 * head_dim]
    return (
        mixed,
        tokens_grad,
        small[:, 2 * head_dim],
        small[:, 2 * head_dim + 1],
        kv_grad,
        w_query_grad,
        w_out_grad,
        w_gate_grad,
        w_up_grad,
        w_down_grad,
    )


def shards_fast(
    tokens,
    segments,
    positions,
    cotangent,
    attn_gain,
    ffn_gain,
    w_kv,
    w_query,
    w_out,
    w_gate,
    w_up,
    w_down,
):
    quarter = w_kv.shape[1] // 8
    lane = jnp.arange(2 * quarter)
    freqs = rope_base ** (-(lane % quarter).astype(jnp.float32) / quarter)
    phase = positions.astype(jnp.float32)[:, None] * freqs[None, :]
    table = (jnp.cos(phase), jnp.where(lane < quarter, -1.0, 1.0)[None, :] * jnp.sin(phase))
    (
        normed_one,
        rotated,
        keys,
        values,
        attn_vals,
        mid,
        normed_two,
        gains,
        allowed,
        kv_weight,
        query_weight,
        out_weight,
        ffn_weights,
        grad_all,
    ) = pre_call(
        tokens,
        w_kv,
        attn_gain[None, :],
        ffn_gain[None, :],
        table,
        segments[None, :],
        cotangent,
        w_query,
        w_out,
        (w_gate, w_up, w_down),
    )
    main = ragged_split(w_gate.shape[1], lax.axis_size("z"))[0]
    grad_mid, gain_part, mix_parts, ffn_sums, grad_mid_low = ffn_call(
        gains, normed_two, grad_all, ffn_weights, mid, w_gate.shape[0], main
    )
    mixed, tokens_grad, gain_grads, kv_grad, query_grad, out_grad, ffn_grads = post_call(
        tokens,
        gains,
        gain_part,
        normed_one,
        rotated,
        keys,
        values,
        attn_vals,
        table,
        allowed,
        kv_weight,
        query_weight,
        out_weight,
        mix_parts,
        grad_mid,
        grad_mid_low,
        mid,
        ffn_sums,
        main,
    )
    *ffn_out, query_grad, out_grad, kv_grad, mixed, tokens_grad = layout_call(
        ffn_sums,
        ffn_grads,
        query_grad,
        out_grad,
        kv_grad,
        mixed,
        tokens_grad,
        w_gate.shape[1],
    )
    share = attn_gain.shape[0]
    place = lax.axis_index(("z", "x", "c", "mp")) * share
    gain_grads = gain_grads.reshape(2, gain_grads.size // 2)
    gain_grads = lax.dynamic_slice(gain_grads, (0, place), (2, share))
    return (
        mixed,
        tokens_grad,
        gain_grads[0],
        gain_grads[1],
        kv_grad,
        query_grad,
        out_grad,
        *ffn_out,
    )


def solution(mesh):
    dp_size, mp_size = mesh.shape["dp"], mesh.shape["mp"]
    if dp_size == 4 * FF_SPLIT and mp_size == 2:
        body, dp = shards_fast, ("z", "x", "c")
        sizes = (FF_SPLIT, 2, 2, mp_size)
    else:
        body, dp = shards_general, ("z", "xc")
        sizes = (FF_SPLIT, dp_size // FF_SPLIT, mp_size)
    all_axes = (*dp, "mp")
    fine = jax.sharding.Mesh(mesh.devices.reshape(sizes), all_axes)
    in_specs = (
        P(all_axes, None),
        P(dp),
        P(dp),
        P(all_axes, None),
        P(all_axes),
        P(all_axes),
        P(all_axes, None),
        P(dp, "mp"),
        P(dp, "mp"),
        P(dp, "mp"),
        P(dp, "mp"),
        P(dp, "mp"),
    )
    out_specs = (
        P(all_axes, None),
        P(all_axes, None),
        P(all_axes),
        P(all_axes),
        P(all_axes, None),
        P(dp, "mp"),
        P(dp, "mp"),
        P(dp, "mp"),
        P(dp, "mp"),
        P(dp, "mp"),
    )
    return jax.shard_map(body, mesh=fine, in_specs=in_specs, out_specs=out_specs, check_vma=False)
```

```python
import functools

import jax
import jax.numpy as jnp
from jax import lax
from jax.experimental import pallas as pl
from jax.experimental.pallas import tpu as pltpu
from jax.sharding import PartitionSpec as P

WINDOW = 2048


epsilon = 1e-06
rope_base = 10000.0
masked_score = -1e30
VMEM_BYTES = 66_000_000


def norm_gain(values, gain):
    return values * lax.rsqrt(jnp.mean(values * values, axis=-1, keepdims=True) + epsilon) * gain


def rotary_angles(positions, head_width):
    quarter = head_width // 4
    freqs = rope_base ** (-jnp.arange(quarter).astype(jnp.float32) / quarter)
    phase = positions.astype(jnp.float32)[:, None] * freqs[None, :]
    return (jnp.cos(phase), jnp.sin(phase))


def rotate(values, cosine, sine):
    quarter = cosine.shape[-1]
    first_half = values[..., :quarter]
    second_half = values[..., quarter : 2 * quarter]
    return jnp.concatenate(
        [
            first_half * cosine - second_half * sine,
            second_half * cosine + first_half * sine,
            values[..., 2 * quarter :],
        ],
        axis=-1,
    )


def unrotate(values, cosine, sine):
    quarter = cosine.shape[-1]
    first_half = values[..., :quarter]
    second_half = values[..., quarter : 2 * quarter]
    return jnp.concatenate(
        [
            first_half * cosine + second_half * sine,
            second_half * cosine - first_half * sine,
            values[..., 2 * quarter :],
        ],
        axis=-1,
    )


def gelu_product(gate, up_proj):
    return jax.nn.gelu(gate, approximate=True) * up_proj


def matmul_nt(left, right):
    return lax.dot_general(
        left, right, (((1,), (1,)), ((), ())), preferred_element_type=jnp.float32
    )


def matmul_tn(left, right):
    return lax.dot_general(
        left, right, (((0,), (0,)), ((), ())), preferred_element_type=jnp.float32
    )


def block_allowed(segments, first_row, rows):
    seq_len = segments.shape[0]
    query_rows = first_row + jnp.arange(rows)
    key_rows = jnp.arange(seq_len)
    return (
        (segments[:, None] == segments[None, :])
        & (key_rows[None, :] <= query_rows[:, None])
        & (query_rows[:, None] - key_rows[None, :] < WINDOW)
    )


MESH_ID = pl.DeviceIdType.MESH
GELU_A = 0.7978845608028654
GELU_B = 0.044715
TILE = 256
WIDE = 512


def remote(src, dst, send_sem, recv_sem, where):
    return pltpu.make_async_remote_copy(
        src_ref=src,
        dst_ref=dst,
        send_sem=send_sem,
        recv_sem=recv_sem,
        device_id=where,
        device_id_type=MESH_ID,
    )


class Halves:
    def __init__(self, src, dst, send_sem, recv_sem, where):
        rows = src.shape[0] // 2
        cuts = [pl.ds(part * rows, rows) for part in range(2)]
        self.copies = [
            remote(src.at[cut], dst.at[cut], send_sem.at[part], recv_sem.at[part], where)
            for part, cut in enumerate(cuts)
        ]

    def start(self):
        for copy in self.copies:
            copy.start()

    def wait_recv(self):
        for copy in self.copies:
            copy.wait_recv()

    def wait_send(self):
        for copy in self.copies:
            copy.wait_send()


def dot_nn(left, right):
    return lax.dot_general(
        left, right, (((1,), (0,)), ((), ())), preferred_element_type=jnp.float32
    )


def gelu_parts(gate):
    square = gate * gate
    bend = jnp.tanh(GELU_A * gate * (1.0 + GELU_B * square))
    half = 0.5 * (1.0 + bend)
    slope = half + 0.5 * gate * (1.0 - bend * bend) * GELU_A * (1.0 + 3.0 * GELU_B * square)
    return gate * half, slope


def add_rows(first, rest, out, count):
    def body(index, carry):
        step = pl.ds(pl.multiple_of(index * 32, 32), 32)
        total = first[step, :].astype(jnp.float32)
        for other in rest:
            total = total + other[step, :].astype(jnp.float32)
        out[step, :] = total.astype(out.dtype)
        return carry

    lax.fori_loop(0, count // 32, body, 0)


def norm_back(values, gain, upstream):
    scale = lax.rsqrt(jnp.mean(values * values, axis=-1, keepdims=True) + epsilon)
    normed = values * scale
    pulled = gain * upstream
    back = scale * (pulled - normed * jnp.mean(normed * pulled, axis=-1, keepdims=True))
    return back, jnp.sum(upstream * normed, axis=0, keepdims=True)


def ffn_kernel(
    z_size,
    main,
    gain_ref,
    own_hbm,
    dy_hbm,
    w_hbm,
    mid_hbm,
    gm_ref,
    gain_part,
    mix_hbm,
    sums_hbm,
    gm_hbm,
    n2,
    dy,
    w3,
    h3,
    n2_t,
    dy_t,
    gn_part,
    mix_buf,
    gn_y,
    gn_z,
    gn_s,
    c_in,
    x_in,
    mid,
    load_sem,
    mix_sem,
    ag_y_send,
    ag_y_recv,
    ag_z_send,
    ag_z_recv,
    rs_y_send,
    rs_y_recv,
    rs_z_send,
    rs_z_recv,
    c_send,
    c_recv,
    x_send,
    x_recv,
    out_sem,
):
    own = own_hbm.shape[0] // 2
    width = own_hbm.shape[1]
    units = w3.shape[2]
    rows = c_in.shape[3]
    span = width // z_size
    me_y, me_z = lax.axis_index("mp"), lax.axis_index("z")
    me_x, me_c = lax.axis_index("x"), lax.axis_index("c")
    mine = pl.ds(pl.multiple_of(me_y * own, own), own)
    theirs = pl.ds(pl.multiple_of((1 - me_y) * own, own), own)
    to_y, to_x, to_c = {"mp": 1 - me_y}, {"x": 1 - me_x}, {"c": 1 - me_c}

    def ahead(step):
        return lax.rem(me_z + step, z_size)

    def to_z(step):
        return {"z": ahead(step)}

    def row_block(z_at, x_at, c_at):
        return pl.ds(pl.multiple_of(((z_at * 2 + x_at) * 2 + c_at) * rows, rows), rows)

    inner = (me_z > 0) & (me_z < z_size - 1)
    outer = (me_z == 0) | (me_z == z_size - 1)

    def w_load(index, columns):
        cols = pl.ds(0, columns)
        return pltpu.make_async_copy(
            w_hbm.at[index, :, cols], w3.at[index, :, cols], load_sem.at[z_size + index]
        )

    def w_loads(act):
        for case, columns in ((inner, units), (outer, main)):

            @pl.when(case)
            def _(columns=columns):
                for index in range(3):
                    act(w_load(index, columns))

    w_loads(lambda copy: copy.start())
    dy_loads = [
        pltpu.make_async_copy(dy_hbm.at[index], dy, load_sem.at[index])
        for index in range(z_size)
    ]
    own_load = pltpu.make_async_copy(own_hbm, n2.at[0], load_sem.at[z_size + 3])
    mid_load = pltpu.make_async_copy(mid_hbm, mid, load_sem.at[z_size + 4])
    for load in (own_load, dy_loads[0], mid_load):
        load.start()

    barrier = pltpu.get_barrier_semaphore()
    peers = [to_y, to_x, to_c] + [to_z(step) for step in range(1, z_size)]
    for where in peers:
        pl.semaphore_signal(barrier, inc=1, device_id=where, device_id_type=MESH_ID)
    pl.semaphore_wait(barrier, len(peers))

    def ag_y(index):
        block = n2.at[index, mine]
        return Halves(block, block, ag_y_send.at[index], ag_y_recv.at[index], to_y)

    def ag_y_in(index):
        block = n2.at[index, theirs]
        return Halves(block, block, ag_y_send.at[index], ag_y_recv.at[index], to_y)

    def ag_z(index):
        src = own_hbm.at[mine] if index == 0 else n2.at[index, mine]
        return Halves(
            src, n2.at[index + 1, mine], ag_z_send.at[index], ag_z_recv.at[index + 1], to_z(1)
        )

    def ag_z_in(index):
        block = n2.at[index, mine]
        return Halves(block, block, ag_z_send.at[0], ag_z_recv.at[index], to_z(1))

    left, right = pl.ds(0, width // 2), pl.ds(width // 2, width // 2)

    def ag_last_z():
        return remote(
            n2.at[2, theirs, left],
            n2.at[3, theirs, left],
            ag_y_send.at[0, 0],
            ag_y_recv.at[0, 0],
            to_z(1),
        )

    def ag_last_y():
        block = n2.at[3, mine, right]
        return remote(block, block, ag_y_send.at[3, 0], ag_y_recv.at[3, 0], to_y)

    def ag_last_y_in():
        block = n2.at[3, theirs, right]
        return remote(block, block, ag_y_send.at[3, 0], ag_y_recv.at[3, 0], to_y)

    def forward(index):
        ag_z_in(index).wait_recv()
        ag_z(index).start()
        ag_y(index).start()

    ag_z(0).start()

    mix_copies = []

    def turn(source, target, index):
        def turn_tile(tile, carry):
            at = pl.ds(pl.multiple_of(tile * span, 128), span)
            target[at, pl.ds(index * 2 * own, 2 * own)] = source[:, at].T
            return carry

        lax.fori_loop(0, z_size, turn_tile, 0)

    def chunk(index):
        if index:
            mix_copies[index - 1].wait()
        dy_loads[index].wait()
        rows_at = pl.ds(index * 2 * own, 2 * own)

        def up_tile(tile, carry):
            cols = pl.ds(pl.multiple_of(tile * WIDE, WIDE), WIDE)
            gate = dot_nn(n2[index], w3[0, :, cols])
            up_proj = dot_nn(n2[index], w3[1, :, cols])
            grad_hidden = dot_nn(dy[...], w3[2, :, cols])
            act, slope = gelu_parts(gate)
            h3[0, rows_at, cols] = (grad_hidden * up_proj * slope).astype(jnp.bfloat16)
            h3[1, rows_at, cols] = (grad_hidden * act).astype(jnp.bfloat16)
            h3[2, rows_at, cols] = (act * up_proj).astype(jnp.bfloat16)
            return carry

        lax.fori_loop(0, units // WIDE, up_tile, 0)

        def down_tile(tile, carry):
            at = pl.ds(pl.multiple_of(tile * span, 128), span)
            normed = matmul_nt(w3[0, at, :], h3[0, rows_at, :]) + matmul_nt(
                w3[1, at, :], h3[1, rows_at, :]
            )
            mixed = matmul_nt(w3[2, at, :], h3[2, rows_at, :])
            for half in range(2):
                cols = slice(half * own, (half + 1) * own)
                gn_part[index, half, at, :] = normed[:, cols].astype(jnp.bfloat16)
                mix_buf[half, at, :] = mixed[:, cols].astype(jnp.bfloat16)
            return carry

        lax.fori_loop(0, z_size, down_tile, 0)
        copy = pltpu.make_async_copy(mix_buf, mix_hbm.at[index], mix_sem.at[index])
        copy.start()
        mix_copies.append(copy)
        if index:
            rs_y(index).start()
        turn(n2.at[index], n2_t, index)
        turn(dy, dy_t, index)
        if index + 1 < z_size:
            dy_loads[index + 1].start()

    def rs_y(index):
        return Halves(
            gn_part.at[index, 1 - me_y], gn_y.at[index], rs_y_send.at[index], rs_y_recv.at[index], to_y
        )

    def rs_z(index):
        return Halves(
            gn_s.at[index - 1],
            gn_z.at[index - 1],
            rs_z_send.at[index],
            rs_z_recv.at[index - 1],
            to_z(1),
        )

    def rs_step(index):
        rs_y(index).wait_recv()
        slot = (index - 2) % z_size
        if index != 1:
            Halves(
                gn_s.at[slot], gn_z.at[slot], rs_z_send.at[1], rs_z_recv.at[slot], to_z(1)
            ).wait_recv()

        def add_tile(tile, carry):
            at = pl.ds(pl.multiple_of(tile * TILE, TILE), TILE)
            total = gn_part[index, me_y, at, :].astype(jnp.float32) + gn_y[index, at, :].astype(
                jnp.float32
            )
            if index != 1:
                total = total + gn_z[slot, at, :].astype(jnp.float32)
            if index == 0:
                gm_ref[:, at] = total.T
            else:
                gn_s[index - 1, at, :] = total.astype(jnp.bfloat16)
            return carry

        lax.fori_loop(0, width // TILE, add_tile, 0)
        if index != 0:
            rs_z(index).start()


    def grads(step):
        at = pl.ds(pl.multiple_of(ahead(step) * span, 128), span)
        for kind, source in enumerate((n2_t, n2_t, dy_t)):

            def tile_body(tile, carry, kind=kind, source=source):
                cols = pl.ds(pl.multiple_of(tile * WIDE, WIDE), WIDE)
                w3[kind, at, cols] = dot_nn(source[at, :], h3[kind, :, cols]).astype(jnp.bfloat16)
                return carry

            lax.fori_loop(0, units // WIDE, tile_body, 0)
            for far in (1, 0):
                over_c(kind, step, far).start()

    def over_c(kind, step, far):
        x_at = 1 - me_x if far else me_x
        return remote(
            w3.at[kind, row_block(ahead(step), x_at, 1 - me_c)],
            c_in.at[kind, step, far],
            c_send.at[kind, step, far],
            c_recv.at[kind, step, far],
            to_c,
        )

    def over_x(kind):
        return remote(
            w3.at[kind, row_block(ahead(1), 1 - me_x, me_c)],
            x_in.at[kind],
            x_send.at[kind],
            x_recv.at[kind],
            to_x,
        )

    out_copies = []

    def keep(kind, step, far, block):
        copy = pltpu.make_async_copy(
            block, sums_hbm.at[kind, step, far], out_sem.at[kind, step, far]
        )
        copy.start()
        out_copies.append(copy)

    def core_sums(step):
        pairs = [(kind, far) for kind in range(3) for far in (1, 0)]
        if step == 1:
            pairs.sort(key=lambda pair: -pair[1])
        for kind, far in pairs:
            over_c(kind, step, far).wait_recv()
            x_at = 1 - me_x if far else me_x
            block = w3.at[kind, row_block(ahead(step), x_at, me_c)]
            add_rows(block, [c_in.at[kind, step, far]], block, rows)
            if step != 1:
                keep(kind, step, far, block)
            elif far:
                over_x(kind).start()

    def first_sums():
        for kind in range(3):
            over_x(kind).wait_recv()
            block = w3.at[kind, row_block(ahead(1), me_x, me_c)]
            add_rows(block, [x_in.at[kind]], block, rows)
            keep(kind, 1, 0, block)

    own_load.wait()
    w_loads(lambda copy: copy.wait())

    @pl.when(outer)
    def _():
        w3[:, :, main:] = jnp.zeros((3, width, units - main), jnp.bfloat16)

    chunk(0)
    forward(1)
    forward(2)
    ag_y_in(1).wait_recv()
    chunk(1)
    ag_y_in(2).wait_recv()
    ag_last_z().start()
    ag_z_in(3).wait_recv()
    ag_last_y().start()
    chunk(2)
    rs_step(1)
    ag_last_z().wait_recv()
    ag_last_y_in().wait_recv()
    chunk(3)
    rs_y(0).start()
    rs_step(2)
    grads(1)
    grads(2)
    core_sums(1)
    rs_step(3)
    grads(3)
    core_sums(2)
    grads(0)
    core_sums(3)
    rs_step(0)
    core_sums(0)

    cot_load = pltpu.make_async_copy(
        dy_hbm.at[0, mine], dy.at[pl.ds(0, own)], load_sem.at[z_size + 3]
    )
    cot_load.start()
    cot_load.wait()
    mid_load.wait()

    def mid_rows(index, total):
        at = pl.ds(pl.multiple_of(index * 32, 32), 32)
        grad, gain_sum = norm_back(mid[at, :], gain_ref[1:2, :], gm_ref[at, :])
        grad = grad + dy[at, :].astype(jnp.float32)
        gm_ref[at, :] = grad
        dy[pl.ds(pl.multiple_of(own + index * 32, 32), 32), :] = grad.astype(jnp.bfloat16)
        return total + gain_sum

    gain_sum = lax.fori_loop(0, own // 32, mid_rows, jnp.zeros((1, width), jnp.float32))
    gm_save = pltpu.make_async_copy(dy.at[pl.ds(own, own)], gm_hbm, load_sem.at[z_size + 3])
    gm_save.start()
    for index in range(4):
        gain_part[index : index + 1, :] = jnp.zeros((1, span), jnp.float32)
        gain_part[4 + index : 5 + index, :] = gain_sum[:, index * span : (index + 1) * span]
    first_sums()
    gm_save.wait()

    for copy in mix_copies[3:] + out_copies:
        copy.wait()
    for index in range(z_size):
        if index in (1, 2):
            ag_y(index).wait_send()
        if index == 3:
            ag_last_z().wait_send()
            ag_last_y().wait_send()
        rs_y(index).wait_send()
        if index < z_size - 1:
            ag_z(index).wait_send()
        if index:
            rs_z(index).wait_send()
        for kind in range(3):
            over_c(kind, index, 0).wait_send()
            over_c(kind, index, 1).wait_send()
            if index == 1:
                over_x(kind).wait_send()


def ffn_call(gains, normed, grad_all, weights, mid, rows, main):
    z_size = lax.axis_size("z")
    pair, width = normed.shape
    units = weights.shape[2]
    own = pair // 2
    wide = lambda *lead: pltpu.VMEM((*lead, width), jnp.bfloat16)
    tall = lambda *lead: pltpu.VMEM((*lead, width, own), jnp.bfloat16)
    dma = lambda *lead: pltpu.SemaphoreType.DMA(lead)
    vmem = pl.BlockSpec(memory_space=pltpu.VMEM)
    hbm = pl.BlockSpec(memory_space=pl.ANY)
    return pl.pallas_call(
        functools.partial(ffn_kernel, z_size, main),
        out_shape=(
            jax.ShapeDtypeStruct((own, width), jnp.float32),
            jax.ShapeDtypeStruct((8, width // z_size), jnp.float32),
            jax.ShapeDtypeStruct((z_size, 2, width, own), jnp.bfloat16),
            jax.ShapeDtypeStruct((3, z_size, 2, rows, units), jnp.bfloat16),
            jax.ShapeDtypeStruct((own, width), jnp.bfloat16),
        ),
        in_specs=[vmem, hbm, hbm, hbm, hbm],
        out_specs=(vmem, vmem, hbm, hbm, hbm),
        scratch_shapes=[
            wide(z_size, pair),
            wide(pair),
            pltpu.VMEM(weights.shape, jnp.bfloat16),
            pltpu.VMEM((3, z_size * pair, units), jnp.bfloat16),
            pltpu.VMEM((width, z_size * pair), jnp.bfloat16),
            pltpu.VMEM((width, z_size * pair), jnp.bfloat16),
            tall(z_size, 2),
            tall(2),
            tall(z_size),
            tall(z_size - 1),
            tall(z_size - 1),
            pltpu.VMEM((3, z_size, 2, rows, units), jnp.bfloat16),
            pltpu.VMEM((3, rows, units), jnp.bfloat16),
            pltpu.VMEM((own, width), jnp.float32),
            dma(z_size + 5),
            dma(z_size),
            dma(z_size, 2),
            dma(z_size, 2),
            dma(z_size, 2),
            dma(z_size, 2),
            dma(z_size, 2),
            dma(z_size, 2),
            dma(z_size, 2),
            dma(z_size, 2),
            dma(3, z_size, 2),
            dma(3, z_size, 2),
            dma(3),
            dma(3),
            dma(3, z_size, 2),
        ],
        compiler_params=pltpu.CompilerParams(
            collective_id=0, has_side_effects=True, vmem_limit_bytes=VMEM_BYTES
        ),
        cost_estimate=pl.CostEstimate(
            flops=18 * z_size * pair * width * units,
            bytes_accessed=4 * weights.size + 12 * z_size * pair * width,
            transcendentals=z_size * pair * units,
        ),
    )(gains, normed, grad_all, weights, mid)


def spin(values, table):
    first = values[:, : values.shape[1] // 2]
    turned = first * table[0] + pltpu.roll(first, first.shape[1] // 2, 1) * table[1]
    return jnp.concatenate([turned, values[:, values.shape[1] // 2 :]], axis=1)


def spin_back(values, table):
    first = values[:, : values.shape[1] // 2]
    turned = first * table[0] - pltpu.roll(first, first.shape[1] // 2, 1) * table[1]
    return jnp.concatenate([turned, values[:, values.shape[1] // 2 :]], axis=1)


def head_probs(rotated, keys, allowed):
    scores = jnp.where(allowed > 0.5, matmul_nt(rotated, keys), masked_score)
    weights = jnp.exp(scores - jnp.max(scores, axis=-1, keepdims=True))
    return weights / jnp.sum(weights, axis=-1, keepdims=True)


def ragged_split(columns, parts):
    main = columns // parts // 128 * 128
    return main, main + 128


def pre_kernel(
    z_size,
    tok_ref,
    wkv_ref,
    gain_one_ref,
    gain_two_ref,
    cos_ref,
    sin_ref,
    seg_ref,
    cot_hbm,
    wq_hbm,
    wo_hbm,
    wg_hbm,
    wu_hbm,
    wd_hbm,
    n1_ref,
    rot_ref,
    key_ref,
    val_ref,
    att_ref,
    mid_ref,
    n2_ref,
    gain_ref,
    allow_ref,
    kv_out,
    wq_out,
    wo_out,
    w3_out,
    dy_out,
    kv_w,
    q_w,
    o_w,
    tok,
    part,
    part_y,
    query,
    gain_rows,
    y_send,
    y_recv,
    ky_send,
    ky_recv,
    az_send,
    az_recv,
    ax_send,
    ax_recv,
    ac_send,
    ac_recv,
    fz_send,
    fz_recv,
    fx_send,
    fx_recv,
    fc_send,
    fc_recv,
    dz_send,
    dz_recv,
    dy_send,
    dy_recv,
    local_sem,
):
    me_z, me_x = lax.axis_index("z"), lax.axis_index("x")
    me_c, me_y = lax.axis_index("c"), lax.axis_index("mp")
    own, width = tok_ref.shape
    rows = wq_hbm.shape[0]
    half_rows = wkv_ref.shape[0]
    head = key_ref.shape[1]
    main, units = ragged_split(wg_hbm.shape[1], z_size)
    to_y, to_x, to_c = {"mp": 1 - me_y}, {"x": 1 - me_x}, {"c": 1 - me_c}

    def to_z(step):
        return {"z": lax.rem(me_z + step, z_size)}

    def from_z(step):
        return lax.rem(me_z - step + z_size, z_size)

    def row_block(step, x_at, c_at):
        start = ((from_z(step) * 2 + x_at) * 2 + c_at) * rows
        return pl.ds(pl.multiple_of(start, rows), rows)

    mine = pl.ds(pl.multiple_of(me_y * own, own), own)
    theirs = pl.ds(pl.multiple_of((1 - me_y) * own, own), own)
    bufs = (kv_w, q_w, o_w)
    inputs = (None, wq_hbm, wo_hbm)

    locals_ = []

    def local(src, dst):
        copy = pltpu.make_async_copy(src, dst, local_sem.at[len(locals_)])
        copy.start()
        locals_.append(copy)
        return copy

    here = row_block(0, me_x, me_c)
    own_q = local(wq_hbm, q_w.at[here])
    own_o = local(wo_hbm, o_w.at[here])
    ffn_in = (wg_hbm, wu_hbm, wd_hbm)

    def body_of(target):
        return pl.ds(pl.multiple_of(target * main, 128), main), pl.ds(0, main)

    def tail_of(target):
        start = z_size * main + lax.rem(target + 1, 2) * 128
        return pl.ds(pl.multiple_of(start, 128), 128), pl.ds(main, 128)

    def is_inner(at):
        return (at > 0) & (at < z_size - 1)

    own_f = []
    for kind in range(3):
        src, dst = body_of(me_z)
        own_f.append(local(ffn_in[kind].at[:, src], w3_out.at[kind, here, dst]))

    def own_tail(kind):
        src, dst = tail_of(me_z)
        return pltpu.make_async_copy(
            ffn_in[kind].at[:, src], w3_out.at[kind, here, dst], local_sem.at[12 + kind]
        )

    @pl.when(is_inner(me_z))
    def _():
        for kind in range(3):
            own_tail(kind).start()
    own_d = local(cot_hbm, dy_out.at[0, mine])

    kv_own = pl.ds(pl.multiple_of(here.start + me_y * half_rows, half_rows), half_rows)
    gain_rows[...] = jnp.zeros(gain_rows.shape, jnp.float32)
    gain_rows[0:1, :half_rows] = gain_one_ref[...].astype(jnp.float32)
    gain_rows[1:2, :half_rows] = gain_two_ref[...].astype(jnp.float32)
    spread = gain_rows[...].T
    kv_w[kv_own, : 2 * head] = wkv_ref[...]
    kv_w[kv_own, 2 * head :] = spread[:half_rows, :].astype(jnp.bfloat16)

    barrier = pltpu.get_barrier_semaphore()
    peers = [to_y, to_x, to_c] + [to_z(step) for step in range(1, z_size)]
    for where in peers:
        pl.semaphore_signal(barrier, inc=1, device_id=where, device_id_type=MESH_ID)
    pl.semaphore_wait(barrier, len(peers))

    tok_y = remote(tok_ref, tok.at[mine], y_send.at[1], y_recv.at[1], to_y)
    tok_y_in = remote(tok_ref, tok.at[theirs], y_send.at[1], y_recv.at[1], to_y)
    part_out = remote(part.at[theirs], part_y, y_send.at[2], y_recv.at[2], to_y)
    n2_y = remote(n2_ref.at[mine], n2_ref.at[mine], y_send.at[3], y_recv.at[3], to_y)
    n2_y_in = remote(n2_ref.at[theirs], n2_ref.at[theirs], y_send.at[3], y_recv.at[3], to_y)

    def block_of(kind, step, x_at):
        if kind:
            return row_block(step, x_at, me_c)
        return kv_rows(step, x_at, me_y)

    def kv_rows(step, x_at, y_at):
        start = row_block(step, x_at, me_c).start + y_at * half_rows
        return pl.ds(pl.multiple_of(start, half_rows), half_rows)

    def kv_y(step, far):
        x_at = 1 - me_x if far else me_x
        block = kv_w.at[kv_rows(step, x_at, me_y)]
        slot = step + z_size * far
        return remote(block, block, ky_send.at[slot], ky_recv.at[slot], to_y)

    def kv_y_in(step, far):
        x_at = 1 - me_x if far else me_x
        block = kv_w.at[kv_rows(step, x_at, 1 - me_y)]
        slot = step + z_size * far
        return remote(block, block, ky_send.at[slot], ky_recv.at[slot], to_y)

    def source(kind, step):
        if isinstance(step, int) and step == 0 and kind:
            return inputs[kind]
        return bufs[kind].at[block_of(kind, step, me_x)]

    first_z, last_z = (z_size - 1 - me_z) // (z_size - 1), me_z // (z_size - 1)
    inner = first_z + last_z == 0
    order = (0, 1 + 2 * first_z, 3 - first_z - last_z, 2 - first_z + last_z)
    hops = (
        None,
        (lax.rem(me_z + 1, z_size), 2),
        (lax.rem(me_z + z_size - 1, z_size), 2),
        (lax.rem(3 * (me_z + 3), z_size), lax.rem(2 * me_z + 3, z_size)),
    )

    def a_z_own(kind, right):
        return remote(
            source(kind, 0),
            bufs[kind].at[block_of(kind, 0, me_x)],
            az_send.at[kind, right],
            az_recv.at[kind, 1 if right else z_size - 1],
            to_z(1 if right else z_size - 1),
        )

    def a_z_start(kind):
        @pl.when(last_z == 0)
        def _():
            a_z_own(kind, 1).start()

        @pl.when(first_z == 0)
        def _():
            a_z_own(kind, 0).start()

    def a_z(kind, index):
        target, slot = hops[index]
        block = bufs[kind].at[block_of(kind, order[index], me_x)]
        return remote(
            block, block, az_send.at[kind, 1 + index], az_recv.at[kind, slot], {"z": target}
        )

    def a_z_next(kind, index):
        @pl.when(inner)
        def _():
            a_z(kind, index).start()

    def a_z_done(kind):
        @pl.when(last_z == 0)
        def _():
            a_z_own(kind, 1).wait_send()

        @pl.when(first_z == 0)
        def _():
            a_z_own(kind, 0).wait_send()

        @pl.when(inner)
        def _():
            for index in range(1, z_size):
                a_z(kind, index).wait_send()

    def a_z_in(kind, step):
        block = bufs[kind].at[block_of(kind, step, me_x)]
        return remote(block, block, az_send.at[kind, 0], az_recv.at[kind, step], to_z(1))

    def a_x(kind, step):
        return remote(
            source(kind, step),
            bufs[kind].at[block_of(kind, step, me_x)],
            ax_send.at[kind, step],
            ax_recv.at[kind, step],
            to_x,
        )

    def a_x_in(kind, step):
        block = bufs[kind].at[block_of(kind, step, 1 - me_x)]
        return remote(block, block, ax_send.at[kind, step], ax_recv.at[kind, step], to_x)

    def a_c(kind, step, far):
        x_at = 1 - me_x if far else me_x
        block = bufs[kind].at[row_block(step, x_at, me_c)]
        src = source(kind, step) if kind and not far else block
        slot = step + z_size * far
        return remote(src, block, ac_send.at[kind, slot], ac_recv.at[kind, slot], to_c)

    def a_c_in(kind, step, far):
        x_at = 1 - me_x if far else me_x
        block = bufs[kind].at[row_block(step, x_at, 1 - me_c)]
        slot = step + z_size * far
        return remote(block, block, ac_send.at[kind, slot], ac_recv.at[kind, slot], to_c)

    def f_z(kind, step, act):
        target = lax.rem(me_z + step, z_size)

        def piece(index, src, dst):
            return remote(
                ffn_in[kind].at[:, src],
                w3_out.at[kind, here, dst],
                fz_send.at[kind, step, index],
                fz_recv.at[kind, step, index],
                to_z(step),
            )

        act(piece(0, *body_of(target)))

        @pl.when(is_inner(target))
        def _():
            act(piece(1, *tail_of(target)))

    def f_z_wait(kind, step):
        block = row_block(step, me_x, me_c)

        def piece(index, dst):
            part = w3_out.at[kind, block, dst]
            return remote(
                part, part, fz_send.at[kind, step, index], fz_recv.at[kind, step, index], to_z(step)
            )

        piece(0, pl.ds(0, main)).wait_recv()

        @pl.when(inner)
        def _():
            piece(1, pl.ds(main, 128)).wait_recv()

    def f_x(kind, step, x_at, act):
        for case, columns in ((inner, units), (first_z + last_z > 0, main)):

            @pl.when(case)
            def _(columns=columns):
                block = w3_out.at[kind, row_block(step, x_at, me_c), pl.ds(0, columns)]
                act(remote(block, block, fx_send.at[kind, step], fx_recv.at[kind, step], to_x))

    def f_x_start(kind, step):
        f_x(kind, step, me_x, lambda copy: copy.start())

    def f_x_wait(kind, step):
        f_x(kind, step, 1 - me_x, lambda copy: copy.wait_recv())

    def f_x_done(kind, step):
        f_x(kind, step, me_x, lambda copy: copy.wait_send())

    def f_c(kind, step, far):
        block = w3_out.at[kind, row_block(step, 1 - me_x if far else me_x, me_c)]
        slot = step + z_size * far
        return remote(block, block, fc_send.at[kind, slot], fc_recv.at[kind, slot], to_c)

    def f_c_in(kind, step, far):
        block = w3_out.at[kind, row_block(step, 1 - me_x if far else me_x, 1 - me_c)]
        slot = step + z_size * far
        return remote(block, block, fc_send.at[kind, slot], fc_recv.at[kind, slot], to_c)

    def d_source(step):
        return cot_hbm if isinstance(step, int) else dy_out.at[step, mine]

    def d_z_own(step):
        return remote(
            cot_hbm, dy_out.at[step, mine], dz_send.at[step], dz_recv.at[step], to_z(step)
        )

    def d_z_next(index):
        return remote(
            dy_out.at[order[index], mine],
            dy_out.at[2, mine],
            dz_send.at[0],
            dz_recv.at[2],
            {"z": hops[index][0]},
        )

    def d_z_all(act):
        @pl.when(inner)
        def _():
            for step in (1, z_size - 1):
                act(d_z_own(step))

        @pl.when(first_z + last_z > 0)
        def _():
            for step in range(1, z_size):
                act(d_z_own(step))

    def d_z_hand(index, act):
        @pl.when(me_z == (2 if index == 1 else 1))
        def _():
            act(d_z_next(index))

    def d_z_done():
        d_z_all(lambda copy: copy.wait_send())
        for index in (1, 2):
            d_z_hand(index, lambda copy: copy.wait_send())

    def d_z_in(step):
        block = dy_out.at[step, mine]
        return remote(block, block, dz_send.at[0], dz_recv.at[step], to_z(1))

    def d_y(step):
        return remote(
            d_source(step), dy_out.at[step, mine], dy_send.at[step], dy_recv.at[step], to_y
        )

    def d_y_in(step):
        block = dy_out.at[step, theirs]
        return remote(block, block, dy_send.at[step], dy_recv.at[step], to_y)

    for kind in (1, 0, 2):
        a_z_start(kind)
        a_x(kind, 0).start()
    kv_y(0, 0).start()
    tok_y.start()
    for kind in (1, 2):
        a_c(kind, 0, 0).start()

    for at_end, away in ((first_z, 1), (last_z, z_size - 1)):

        @pl.when(at_end > 0)
        def _(away=away):
            for step in (z_size - away, 2, away):
                d_z_own(step).start()
            for kind in range(3):
                f_z(kind, away, lambda copy: copy.start())

    tok[mine, :] = tok_ref[...]
    seq = 2 * own
    query_at = lax.broadcasted_iota(jnp.int32, (seq, seq), 0)
    key_at = lax.broadcasted_iota(jnp.int32, (seq, seq), 1)
    segment = seg_ref[...].astype(jnp.float32)
    same = jnp.broadcast_to(segment, (8, seq)).T[:, :1] == segment
    allowed = same & (key_at <= query_at) & (query_at - key_at < WINDOW)
    allow_ref[...] = jnp.where(allowed, 1.0, 0.0)
    d_y(0).start()

    def from_x(index):
        step = order[index]
        for kind in (1, 0, 2):
            a_x_in(kind, step).wait_recv()
            if kind:
                a_c(kind, step, 1).start()
            else:
                kv_y(step, 1).start()

    def from_y(index):
        step = order[index]
        for far in range(2):
            kv_y_in(step, far).wait_recv()
            a_c(0, step, far).start()

    for index in range(1, z_size):
        step = order[index]
        for kind in (1, 0, 2):
            a_z_in(kind, step).wait_recv()
            a_z_next(kind, index)
            a_x(kind, step).start()
            if kind:
                a_c(kind, step, 0).start()
            else:
                kv_y(step, 0).start()
        if index == z_size - 1:

            @pl.when(inner)
            def _():
                for way in (1, z_size - 1):
                    d_z_own(way).start()

            for copy in own_f:
                copy.wait()

            @pl.when(inner)
            def _():
                for kind in range(3):
                    own_tail(kind).wait()

            for kind in range(3):
                for away, sent in ((1, first_z), (3, last_z), (2, 0)):

                    @pl.when(sent == 0 if away != 2 else me_z >= 0)
                    def _(kind=kind, away=away):
                        f_z(kind, away, lambda copy: copy.start())

            for kind in range(3):
                f_x_start(kind, 0)
                f_c(kind, 0, 0).start()
        if index >= 2:
            from_x(index - 2)
            from_y(index - 2)
    def pass_cotangent(index):
        d_z_in(order[index]).wait_recv()
        if index < 3:
            d_z_hand(index, lambda copy: copy.start())
        d_y(order[index]).start()

    def pass_if(case, index):
        @pl.when(case)
        def _():
            pass_cotangent(index)

    outer = first_z + last_z > 0
    pass_cotangent(3)
    from_x(z_size - 2)
    from_y(z_size - 2)
    pass_cotangent(1)
    from_x(z_size - 1)
    from_y(z_size - 1)
    pass_if(inner, 2)

    def hand_on(kind, step):
        f_z_wait(kind, step)
        f_x_start(kind, step)
        f_c(kind, step, 0).start()

    def cross(kind, step):
        f_x_wait(kind, step)
        f_c(kind, step, 1).start()

    tok_y_in.wait_recv()
    own_q.wait()
    own_o.wait()
    for kind in (0, 1):
        for step in range(z_size):
            for far in range(2):
                a_c_in(kind, step, far).wait_recv()

    gains = kv_w[:, 2 * head :].astype(jnp.float32).T[:8, :]
    gain_ref[...] = gains

    def norm_rows(index, carry):
        at = pl.ds(pl.multiple_of(index * 32, 32), 32)
        values = tok[at, :].astype(jnp.float32)
        scale = lax.rsqrt(jnp.mean(values * values, axis=-1, keepdims=True) + epsilon)
        n1_ref[at, :] = (values * scale * gain_ref[0:1, :]).astype(jnp.bfloat16)
        return carry

    lax.fori_loop(0, 2 * own // 32, norm_rows, 0)
    hand_on(0, order[1])
    table = (cos_ref[...], sin_ref[...])
    key_ref[...] = spin(dot_nn(n1_ref[...], kv_w[:, :head]), table).astype(jnp.bfloat16)
    val_ref[...] = dot_nn(n1_ref[...], kv_w[:, head : 2 * head]).astype(jnp.bfloat16)
    hand_on(0, order[2])
    head_scale = head ** (-0.5)
    heads = att_ref.shape[1] // head

    half_cols = att_ref.shape[1] // 2
    for index in range(2):
        cols = pl.ds(index * half_cols, half_cols)
        query[:, cols] = dot_nn(n1_ref[...], q_w[:, cols])

    def attend(index):
        cols = pl.ds(index * head, head)
        rotated = (spin(query[:, cols], table) * head_scale).astype(jnp.bfloat16)
        rot_ref[:, cols] = rotated
        probs = head_probs(rotated, key_ref[...], allow_ref[...]).astype(jnp.bfloat16)
        att_ref[:, cols] = dot_nn(probs, val_ref[...]).astype(jnp.bfloat16)

    tasks = [
        lambda: hand_on(0, order[3]),
        lambda: (cross(0, 0), hand_on(1, order[1])),
        lambda: cross(1, 0),
        lambda: hand_on(1, order[2]),
        lambda: (cross(2, 0), pass_if(outer, 2)),
    ]
    for index in range(heads):
        attend(index)
        if index < len(tasks):
            tasks[index]()
    for step in range(z_size):
        for far in range(2):
            a_c_in(2, step, far).wait_recv()
    saves = [
        local(kv_w, kv_out),
        local(q_w, wq_out),
        local(o_w, wo_out),
    ]
    span = width // 4

    def project(index, carry):
        cols = pl.ds(pl.multiple_of(index * span, span), span)
        part[:, cols] = matmul_nt(att_ref[...], o_w[cols, :]).astype(jnp.bfloat16)
        return carry

    lax.fori_loop(0, 4, project, 0)
    part_out.start()
    hand_on(1, order[3])
    cross(0, order[1])
    hand_on(2, order[1])
    part_out.wait_recv()

    def middle(index, carry):
        at = pl.ds(pl.multiple_of(index * 32, 32), 32)
        there = pl.ds(pl.multiple_of(me_y * own + index * 32, 32), 32)
        values = (
            tok_ref[at, :].astype(jnp.float32)
            + part[there, :].astype(jnp.float32)
            + part_y[at, :].astype(jnp.float32)
        )
        mid_ref[at, :] = values
        scale = lax.rsqrt(jnp.mean(values * values, axis=-1, keepdims=True) + epsilon)
        n2_ref[there, :] = (values * scale * gain_ref[1:2, :]).astype(jnp.bfloat16)
        return carry

    lax.fori_loop(0, own // 32, middle, 0)
    n2_y.start()
    hand_on(2, order[2])
    cross(0, order[2])
    cross(0, order[3])
    hand_on(2, order[3])
    for kind in (1, 2):
        for index in (1, 2, 3):
            cross(kind, order[index])
    for kind in range(3):
        for step in range(z_size):
            for far in range(2):
                f_c_in(kind, step, far).wait_recv()
    for step in range(z_size):
        d_y_in(step).wait_recv()
    n2_y_in.wait_recv()

    for kind in range(3):
        a_z_done(kind)
    d_z_done()
    tok_y.wait_send()
    part_out.wait_send()
    n2_y.wait_send()
    own_d.wait()
    for copy in saves:
        copy.wait()
    for step in range(z_size):
        d_y(step).wait_send()
        for far in range(2):
            kv_y(step, far).wait_send()
        for kind in range(3):
            if step:
                f_z(kind, step, lambda copy: copy.wait_send())
            a_x(kind, step).wait_send()
            f_x_done(kind, step)
            for far in range(2):
                a_c(kind, step, far).wait_send()
                f_c(kind, step, far).wait_send()


def pre_call(
    tokens, w_kv, gain_one, gain_two, table, segments, cotangent, w_query, w_out, ffn
):
    z_size = lax.axis_size("z")
    own, width = tokens.shape
    seq = 2 * own
    rows, cols = w_query.shape
    head = table[0].shape[1] * 2
    units = ragged_split(ffn[0].shape[1], z_size)[1]
    low = lambda *dims: jax.ShapeDtypeStruct(dims, jnp.bfloat16)
    full = lambda *dims: jax.ShapeDtypeStruct(dims, jnp.float32)
    dma = lambda *lead: pltpu.SemaphoreType.DMA(lead)
    vmem = pl.BlockSpec(memory_space=pltpu.VMEM)
    hbm = pl.BlockSpec(memory_space=pl.ANY)
    wide = lambda *lead: pltpu.VMEM((*lead, width), jnp.bfloat16)
    return pl.pallas_call(
        functools.partial(pre_kernel, z_size),
        out_shape=(
            low(seq, width),
            low(seq, cols),
            low(seq, head),
            low(seq, head),
            low(seq, cols),
            full(own, width),
            low(seq, width),
            full(8, width),
            full(seq, seq),
            low(width, 2 * head + 128),
            low(width, cols),
            low(width, cols),
            low(3, width, units),
            low(z_size, seq, width),
        ),
        in_specs=[vmem] * 7 + [hbm] * 6,
        out_specs=(vmem,) * 9 + (hbm,) * 5,
        scratch_shapes=[
            pltpu.VMEM((width, 2 * head + 128), jnp.bfloat16),
            pltpu.VMEM((width, cols), jnp.bfloat16),
            pltpu.VMEM((width, cols), jnp.bfloat16),
            wide(seq),
            wide(seq),
            wide(own),
            pltpu.VMEM((seq, cols), jnp.float32),
            pltpu.VMEM((128, 128), jnp.float32),
            dma(4),
            dma(4),
            dma(2 * z_size),
            dma(2 * z_size),
            dma(3, z_size + 1),
            dma(3, z_size),
            dma(3, z_size),
            dma(3, z_size),
            dma(3, 2 * z_size),
            dma(3, 2 * z_size),
            dma(3, z_size, 2),
            dma(3, z_size, 2),
            dma(3, z_size),
            dma(3, z_size),
            dma(3, 2 * z_size),
            dma(3, 2 * z_size),
            dma(z_size + 1),
            dma(z_size),
            dma(z_size),
            dma(z_size),
            dma(16),
        ],
        compiler_params=pltpu.CompilerParams(
            collective_id=1, has_side_effects=True, vmem_limit_bytes=VMEM_BYTES
        ),
        cost_estimate=pl.CostEstimate(
            flops=8 * seq * width * cols,
            bytes_accessed=8 * width * (cols + units),
            transcendentals=seq * seq * cols // head,
        ),
    )(tokens, w_kv, gain_one, gain_two, *table, segments, cotangent, w_query, w_out, *ffn)


def post_kernel(
    z_size,
    main,
    tok_ref,
    gain_ref,
    gain_part_ref,
    n1_ref,
    rot_ref,
    key_ref,
    val_ref,
    att_ref,
    cos_ref,
    sin_ref,
    allow_ref,
    kv_hbm,
    wq_hbm,
    wo_hbm,
    mix_hbm,
    gmf_hbm,
    gmb_hbm,
    mid_hbm,
    sums_hbm,
    mixed_ref,
    tgrad_ref,
    gsum_ref,
    kvg_ref,
    qg_ref,
    og_ref,
    ffn_out,
    kv_w,
    q_w,
    o_w,
    o_part,
    gm,
    gm_f,
    gq,
    gkv,
    kv_sum,
    back_y,
    mix_y,
    mix_z,
    mix_s,
    o_c,
    o_x,
    o_z,
    q_c,
    q_x,
    q_z,
    kv_y,
    kv_c,
    kv_x,
    kv_z,
    gain_own,
    gain_in,
    ffn_in,
    ffn_own,
    load_sem,
    own_sem,
    fx_send,
    fx_recv,
    fz_send,
    fz_recv,
    y_send,
    y_recv,
    my_send,
    my_recv,
    mz_send,
    mz_recv,
    wc_send,
    wc_recv,
    wx_send,
    wx_recv,
    wz_send,
    wz_recv,
    kc_send,
    kc_recv,
    kz_send,
    kz_recv,
    g_send,
    g_recv,
):
    me_z, me_x = lax.axis_index("z"), lax.axis_index("x")
    me_c, me_y = lax.axis_index("c"), lax.axis_index("mp")
    own, width = tok_ref.shape
    seq = 2 * own
    head = key_ref.shape[1]
    cols_here = att_ref.shape[1]
    heads = cols_here // head
    rows = qg_ref.shape[0]
    span = width // z_size
    mine = pl.ds(pl.multiple_of(me_y * own, own), own)
    theirs = pl.ds(pl.multiple_of((1 - me_y) * own, own), own)
    to_y, to_x, to_c = {"mp": 1 - me_y}, {"x": 1 - me_x}, {"c": 1 - me_c}
    head_scale = head ** (-0.5)

    def behind(step):
        return lax.rem(me_z - step + z_size, z_size)

    def to_z(step):
        return {"z": lax.rem(me_z + step, z_size)}

    def row_block(step, x_at, c_at):
        start = ((behind(step) * 2 + x_at) * 2 + c_at) * rows
        return pl.ds(pl.multiple_of(start, rows), rows)

    loads = [
        pltpu.make_async_copy(wo_hbm, o_w, load_sem.at[0]),
        pltpu.make_async_copy(wq_hbm, q_w, load_sem.at[1]),
        pltpu.make_async_copy(
            kv_hbm.at[:, :, :, :, :, pl.ds(0, 2 * head)], kv_w, load_sem.at[2]
        ),
    ]
    for step in range(z_size):
        loads.append(
            pltpu.make_async_copy(mix_hbm.at[step, me_y], mix_s.at[step], load_sem.at[3 + step])
        )
    loads.append(pltpu.make_async_copy(gmf_hbm, gm_f, load_sem.at[3 + z_size]))
    loads.append(pltpu.make_async_copy(gmb_hbm, gm.at[mine], load_sem.at[4 + z_size]))
    mid_load = pltpu.make_async_copy(mid_hbm, gm_f, load_sem.at[5 + z_size])
    for load in loads:
        load.start()

    barrier = pltpu.get_barrier_semaphore()
    peers = [to_y, to_x, to_c] + [to_z(step) for step in range(1, z_size)]
    for where in peers:
        pl.semaphore_signal(barrier, inc=1, device_id=where, device_id_type=MESH_ID)
    pl.semaphore_wait(barrier, len(peers))

    tasks = [(step, kind) for step in (2, 3) for kind in range(3)]

    def f_x(index):
        step, kind = tasks[index]
        return remote(
            sums_hbm.at[kind, step, 1],
            ffn_in.at[index],
            fx_send.at[index],
            fx_recv.at[index],
            to_x,
        )

    def f_own(index):
        step, kind = tasks[index]
        return pltpu.make_async_copy(
            sums_hbm.at[kind, step, 0], ffn_own.at[index % 2], own_sem.at[index % 2]
        )

    def f_z(step, kind, source_z, act):
        for case, columns in (
            ((source_z > 0) & (source_z < z_size - 1), ffn_out.shape[3]),
            ((source_z == 0) | (source_z == z_size - 1), main),
        ):

            @pl.when(case)
            def _(columns=columns):
                cols = pl.ds(0, columns)
                if step == 1:
                    src = sums_hbm.at[kind, 1, 0, :, cols]
                else:
                    src = ffn_in.at[tasks.index((step, kind)), :, cols]
                act(
                    remote(
                        src,
                        ffn_out.at[kind, step, :, cols],
                        fz_send.at[kind, step],
                        fz_recv.at[kind, step],
                        to_z(step),
                    )
                )

    def tick(index):
        step, kind = tasks[index]
        f_x(index).wait_recv()
        f_own(index).wait()
        block = ffn_in.at[index]
        add_rows(block, [ffn_own.at[index % 2]], block, rows)
        if index + 2 < len(tasks):
            f_own(index + 2).start()
        f_z(step, kind, me_z, lambda copy: copy.start())

    def f_x_own(kind):
        return remote(
            sums_hbm.at[kind, 0, 1],
            ffn_out.at[kind, 0],
            fx_send.at[len(tasks) + kind],
            fx_recv.at[len(tasks) + kind],
            to_x,
        )

    f_own(0).start()
    f_own(1).start()
    for index in range(len(tasks)):
        f_x(index).start()
    for kind in range(3):
        f_z(1, kind, me_z, lambda copy: copy.start())

    gm_y = remote(gmb_hbm, gm.at[mine], y_send.at[0], y_recv.at[0], to_y)
    gm_y_in = remote(gm.at[theirs], gm.at[theirs], y_send.at[0], y_recv.at[0], to_y)
    gm_y.start()

    first_z, last_z = (z_size - 1 - me_z) // (z_size - 1), me_z // (z_size - 1)
    inner = first_z + last_z == 0
    order = (
        0,
        1 + (me_z + 1) // 2,
        2 + (2 * me_z - 3) * (1 - first_z - last_z),
        3 - 2 * (me_z // 2),
    )
    right = (None, 1 - me_z // 2, (3 - me_z) * (2 - me_z) // 6 + me_z // 2 * (1 - last_z), 1 - me_z // 2)

    def hop_slot(index):
        step, way = order[index], right[index]
        return way * lax.rem(step + 1, z_size) + (1 - way) * (step - 1 + 4 * ((3 - step) // 2))

    def hop_target(index):
        return {"z": me_z + 2 * right[index] - 1}

    def mix_over_y(step):
        return remote(
            mix_hbm.at[step, 1 - me_y], mix_y.at[step], my_send.at[step], my_recv.at[step], to_y
        )

    def mix_over_z(index):
        slot = hop_slot(index)
        return remote(
            mix_s.at[order[index]],
            mix_z.at[slot],
            mz_send.at[index],
            mz_recv.at[slot],
            hop_target(index),
        )

    def mix_z_in(slot):
        return remote(mix_z.at[slot], mix_z.at[slot], mz_send.at[1], mz_recv.at[slot], to_z(1))

    def mix_add(step, others, last):
        def add_tile(tile, carry):
            at = pl.ds(pl.multiple_of(tile * TILE, TILE), TILE)
            total = mix_s[step, at, :].astype(jnp.float32)
            for other in others:
                total = total + other[at, :].astype(jnp.float32)
            if last:
                mixed_ref[:, at] = (gm_f[:, at] + total.T).astype(jnp.bfloat16)
            else:
                mix_s[step, at, :] = total.astype(jnp.bfloat16)
            return carry

        lax.fori_loop(0, width // TILE, add_tile, 0)

    def mix_step(index):
        step = order[index]
        mix_over_y(step).wait_recv()
        from_y = mix_y.at[step]
        if index:

            @pl.when(inner)
            def _():
                mix_z_in(step).wait_recv()
                mix_add(step, [from_y, mix_z.at[step]], False)

            @pl.when(first_z + last_z > 0)
            def _():
                mix_add(step, [from_y], False)

            mix_over_z(index).start()
        else:
            mid_load.wait()

            @pl.when(first_z == 0)
            def _():
                mix_z_in(0).wait_recv()

            @pl.when(last_z == 0)
            def _():
                mix_z_in(z_size).wait_recv()

            @pl.when(inner)
            def _():
                mix_add(0, [from_y, mix_z.at[0], mix_z.at[z_size]], True)

            @pl.when(first_z > 0)
            def _():
                mix_add(0, [from_y, mix_z.at[z_size]], True)

            @pl.when(last_z > 0)
            def _():
                mix_add(0, [from_y, mix_z.at[0]], True)

    for index in (1, 2, 3, 0):
        mix_over_y(order[index]).start()

    kinds = ((o_part, o_c, o_x, o_z, og_ref), (o_w, q_c, q_x, q_z, qg_ref))

    def w_c(kind, step, far):
        x_at = 1 - me_x if far else me_x
        return remote(
            kinds[kind][0].at[row_block(step, x_at, 1 - me_c)],
            kinds[kind][1].at[step, far],
            wc_send.at[kind, step, far],
            wc_recv.at[kind, step, far],
            to_c,
        )

    def w_x(kind, step):
        return remote(
            kinds[kind][0].at[row_block(step, 1 - me_x, me_c)],
            kinds[kind][2].at[step],
            wx_send.at[kind, step],
            wx_recv.at[kind, step],
            to_x,
        )

    def w_z(kind, index):
        step, slot = order[index], hop_slot(index)
        return remote(
            kinds[kind][0].at[row_block(step, me_x, me_c)],
            kinds[kind][3].at[slot],
            wz_send.at[kind, index],
            wz_recv.at[kind, slot],
            hop_target(index),
        )

    def w_z_in(kind, slot):
        block = kinds[kind][3].at[slot]
        return remote(block, block, wz_send.at[kind, 1], wz_recv.at[kind, slot], to_z(1))

    def w_x_stage(kind, index):
        step = order[index]
        w_c(kind, step, 1).wait_recv()
        block = kinds[kind][0].at[row_block(step, 1 - me_x, me_c)]
        add_rows(block, [kinds[kind][1].at[step, 1]], block, rows)
        w_x(kind, step).start()

    def w_z_stage(kind, index):
        part, from_c, from_x, from_z, result = kinds[kind]
        step = order[index]
        w_c(kind, step, 0).wait_recv()
        w_x(kind, step).wait_recv()
        block = part.at[row_block(step, me_x, me_c)]
        others = [from_c.at[step, 0], from_x.at[step]]
        if index:

            @pl.when(inner)
            def _():
                w_z_in(kind, step).wait_recv()
                add_rows(block, [*others, from_z.at[step]], block, rows)

            @pl.when(first_z + last_z > 0)
            def _():
                add_rows(block, others, block, rows)

            w_z(kind, index).start()
        else:

            @pl.when(first_z == 0)
            def _():
                w_z_in(kind, 0).wait_recv()

            @pl.when(last_z == 0)
            def _():
                w_z_in(kind, z_size).wait_recv()

            @pl.when(inner)
            def _():
                add_rows(block, [*others, from_z.at[0], from_z.at[z_size]], result, rows)

            @pl.when(first_z > 0)
            def _():
                add_rows(block, [*others, from_z.at[z_size]], result, rows)

            @pl.when(last_z > 0)
            def _():
                add_rows(block, [*others, from_z.at[0]], result, rows)

    def w_product(kind, index, left, values):
        step = order[index]
        at = pl.ds(pl.multiple_of(behind(step) * span, 128), span)
        turned = left[:, at].T

        def tile_body(tile, carry):
            cols = pl.ds(pl.multiple_of(tile * TILE, TILE), TILE)
            kinds[kind][0][at, cols] = dot_nn(turned, values[:, cols]).astype(jnp.bfloat16)
            return carry

        lax.fori_loop(0, cols_here // TILE, tile_body, 0)
        for far in (1, 0):
            w_c(kind, step, far).start()

    tick(0)
    tick(1)
    loads[-1].wait()
    gm_y_in.wait_recv()
    w_product(0, 1, gm, att_ref)
    w_product(0, 2, gm, att_ref)
    w_x_stage(0, 1)
    w_product(0, 3, gm, att_ref)
    w_x_stage(0, 2)
    tick(2)
    w_product(0, 0, gm, att_ref)
    w_x_stage(0, 3)
    for load in loads[:-1]:
        load.wait()

    kv_sum[...] = jnp.zeros(kv_sum.shape, jnp.float32)
    table = (cos_ref[...], sin_ref[...])

    for index in range(2):
        cols = pl.ds(index * (cols_here // 2), cols_here // 2)
        gq[:, cols] = dot_nn(gm[...], o_w[:, cols]).astype(jnp.bfloat16)

    def attend_back(index):
        cols = pl.ds(index * head, head)
        grad_vals = gq[:, cols]
        rotated = rot_ref[:, cols]
        probs = head_probs(rotated, key_ref[...], allow_ref[...])
        grad_probs = matmul_nt(grad_vals, val_ref[...])
        delta = jnp.sum(probs * grad_probs, axis=-1, keepdims=True)
        grad_scores = (probs * (grad_probs - delta)).astype(jnp.bfloat16)
        grad_rot = dot_nn(grad_scores, key_ref[...])
        gq[:, cols] = (spin_back(grad_rot, table) * head_scale).astype(jnp.bfloat16)
        kv_sum[0] += matmul_tn(grad_scores, rotated)
        kv_sum[1] += matmul_tn(probs.astype(jnp.bfloat16), grad_vals)

    for index in range(heads):
        attend_back(index)
        if index == 0:
            w_x_stage(0, 0)
        if 3 + index < len(tasks):
            tick(3 + index)
        if index == heads - 1:
            mix_step(1)
    gkv[:, :head] = spin_back(kv_sum[0], table).astype(jnp.bfloat16)
    gkv[:, head:] = kv_sum[1].astype(jnp.bfloat16)

    w_product(1, 1, n1_ref, gq)
    w_product(1, 2, n1_ref, gq)
    w_x_stage(1, 1)
    w_z_stage(0, 1)
    w_product(1, 3, n1_ref, gq)
    w_x_stage(1, 2)
    w_product(1, 0, n1_ref, gq)
    w_x_stage(1, 3)
    w_x_stage(1, 0)
    for kind in range(3):
        f_x_own(kind).start()

    gm_y.wait_send()
    back = gm
    def input_tile(index, carry):
        at = pl.ds(pl.multiple_of(index * span, 128), span)
        back[:, at] = (
            matmul_nt(gq[...], q_w[at, :]) + matmul_nt(gkv[...], kv_w[index].reshape(span, 2 * head))
        ).astype(jnp.bfloat16)
        return carry

    lax.fori_loop(0, z_size, input_tile, 0)
    back_out = remote(back.at[theirs], back_y, y_send.at[1], y_recv.at[1], to_y)
    back_out.start()

    kv_part = kv_w

    def kv_tile(index, carry):
        at = pl.ds(pl.multiple_of(index * span, 128), span)
        product = dot_nn(n1_ref[:, at].T, gkv[...]).astype(jnp.bfloat16)
        kv_part[index] = product.reshape(kv_part.shape[1:])
        return carry

    lax.fori_loop(0, z_size, kv_tile, 0)
    kv_over_y = remote(kv_part.at[:, :, :, 1 - me_y], kv_y, y_send.at[2], y_recv.at[2], to_y)
    kv_over_y.start()
    mix_step(2)
    w_z_stage(0, 2)
    mix_step(3)
    w_z_stage(0, 3)

    back_out.wait_recv()

    def input_rows(index, total):
        at = pl.ds(pl.multiple_of(index * 32, 32), 32)
        there = pl.ds(pl.multiple_of(me_y * own + index * 32, 32), 32)
        upstream = back[there, :].astype(jnp.float32) + back_y[at, :].astype(jnp.float32)
        grad, gain_part = norm_back(
            tok_ref[at, :].astype(jnp.float32), gain_ref[0:1, :], upstream
        )
        tgrad_ref[at, :] = (gm_f[at, :] + grad).astype(jnp.bfloat16)
        return total + gain_part

    attn_gain_part = lax.fori_loop(
        0, own // 32, input_rows, jnp.zeros((1, width), jnp.float32)
    )
    for index in range(4):
        at = slice(index * span, (index + 1) * span)
        gain_own[0, index : index + 1, :] = attn_gain_part[:, at]
        gain_own[0, 4 + index : 5 + index, :] = gain_part_ref[4 + index : 5 + index, :]

    def gain_send(stage, where):
        return remote(
            gain_own.at[stage], gain_in.at[stage], g_send.at[stage], g_recv.at[stage], where
        )

    gain_hops = [gain_send(0, to_y), gain_send(1, to_c), gain_send(2, to_x)]
    gain_last = [
        remote(
            gain_own.at[3], gain_in.at[2 + step], g_send.at[2 + step], g_recv.at[2 + step], to_z(step)
        )
        for step in range(1, z_size)
    ]

    def gain_fold(stage):
        gain_hops[stage].wait_recv()
        gain_own[stage + 1] = gain_own[stage] + gain_in[stage]

    gain_hops[0].start()
    mid_load.start()
    w_z_stage(1, 1)
    w_z_stage(0, 0)
    w_z_stage(1, 2)
    gain_fold(0)
    gain_hops[1].start()
    mix_step(0)
    w_z_stage(1, 3)
    gain_fold(1)
    gain_hops[2].start()
    kv_over_y.wait_recv()

    def kv_add_y(index, carry):
        for x_at in range(2):
            for c_at in range(2):
                block = kv_part.at[index, x_at, c_at, me_y]
                block[...] = (
                    block[...].astype(jnp.float32) + kv_y[index, x_at, c_at].astype(jnp.float32)
                ).astype(jnp.bfloat16)
        return carry

    lax.fori_loop(0, z_size, kv_add_y, 0)
    kv_over_c = remote(
        kv_part.at[:, :, 1 - me_c, me_y], kv_c, kc_send.at[0], kc_recv.at[0], to_c
    )
    kv_over_c.start()
    gain_fold(2)
    for copy in gain_last:
        copy.start()
    kv_over_c.wait_recv()

    def kv_add_c(index, carry):
        for x_at in range(2):
            block = kv_part.at[index, x_at, me_c, me_y]
            block[...] = (
                block[...].astype(jnp.float32) + kv_c[index, x_at].astype(jnp.float32)
            ).astype(jnp.bfloat16)
        return carry

    lax.fori_loop(0, z_size, kv_add_c, 0)
    kv_over_x = remote(
        kv_part.at[:, 1 - me_x, me_c, me_y], kv_x, kc_send.at[1], kc_recv.at[1], to_x
    )
    kv_over_x.start()
    w_z_stage(1, 0)
    kv_over_x.wait_recv()

    def kv_add_x(index, carry):
        block = kv_part.at[index, me_x, me_c, me_y]
        block[...] = (
            block[...].astype(jnp.float32) + kv_x[index].astype(jnp.float32)
        ).astype(jnp.bfloat16)
        return carry

    lax.fori_loop(0, z_size, kv_add_x, 0)
    kv_over_z = [
        remote(
            kv_part.at[lax.rem(me_z + step, z_size), me_x, me_c, me_y],
            kv_z.at[step - 1],
            kz_send.at[step],
            kz_recv.at[step],
            to_z(step),
        )
        for step in range(1, z_size)
    ]
    for copy in kv_over_z:
        copy.start()
    for copy in gain_last:
        copy.wait_recv()
    gsum_ref[...] = gain_own[3] + gain_in[3] + gain_in[4] + gain_in[5]
    for copy in kv_over_z:
        copy.wait_recv()
    kvg_ref[...] = (
        kv_part[me_z, me_x, me_c, me_y].astype(jnp.float32)
        + kv_z[0].astype(jnp.float32)
        + kv_z[1].astype(jnp.float32)
        + kv_z[2].astype(jnp.float32)
    )

    back_out.wait_send()
    kv_over_y.wait_send()
    kv_over_c.wait_send()
    kv_over_x.wait_send()
    for kind in range(3):
        f_x_own(kind).wait()
    for index in range(len(tasks)):
        f_x(index).wait_send()
    for step in range(1, z_size):
        for kind in range(3):
            f_z(step, kind, me_z, lambda copy: copy.wait_send())
            f_z(step, kind, behind(step), lambda copy: copy.wait_recv())
    for copy in gain_hops + gain_last + kv_over_z:
        copy.wait_send()
    for step in range(z_size):
        mix_over_y(step).wait_send()
        if step:
            mix_over_z(step).wait_send()
        for kind in range(2):
            w_c(kind, step, 0).wait_send()
            w_c(kind, step, 1).wait_send()
            w_x(kind, step).wait_send()
            if step:
                w_z(kind, step).wait_send()


def post_call(
    tokens,
    gains,
    gain_part,
    normed_one,
    rotated,
    keys,
    values,
    attn_vals,
    table,
    allowed,
    kv_weight,
    query_weight,
    out_weight,
    mix_parts,
    grad_mid,
    grad_mid_low,
    mid,
    ffn_sums,
    main,
):
    z_size = lax.axis_size("z")
    own, width = tokens.shape
    seq = 2 * own
    head = keys.shape[1]
    cols = attn_vals.shape[1]
    rows = width // (4 * z_size)
    units = ffn_sums.shape[4]
    low = lambda *dims: pltpu.VMEM(dims, jnp.bfloat16)
    full = lambda *dims: pltpu.VMEM(dims, jnp.float32)
    out_full = lambda *dims: jax.ShapeDtypeStruct(dims, jnp.float32)
    out_low = lambda *dims: jax.ShapeDtypeStruct(dims, jnp.bfloat16)
    dma = lambda *lead: pltpu.SemaphoreType.DMA(lead)
    vmem = pl.BlockSpec(memory_space=pltpu.VMEM)
    hbm = pl.BlockSpec(memory_space=pl.ANY)
    z = z_size
    return pl.pallas_call(
        functools.partial(post_kernel, z_size, main),
        out_shape=(
            out_low(own, width),
            out_low(own, width),
            out_full(8, width // z),
            out_full(rows // 2, 2 * head),
            out_full(rows, cols),
            out_full(rows, cols),
            out_low(3, z, rows, units),
        ),
        in_specs=[vmem] * 11 + [hbm] * 8,
        out_specs=(vmem,) * 6 + (hbm,),
        scratch_shapes=[
            low(z, 2, 2, 2, rows // 2, 2 * head),
            low(width, cols),
            low(width, cols),
            low(width, cols),
            low(seq, width),
            full(own, width),
            low(seq, cols),
            low(seq, 2 * head),
            full(2, seq, head),
            low(own, width),
            low(z, width, own),
            low(z + 1, width, own),
            low(z, width, own),
            low(z, 2, rows, cols),
            low(z, rows, cols),
            low(z + 1, rows, cols),
            low(z, 2, rows, cols),
            low(z, rows, cols),
            low(z + 1, rows, cols),
            low(z, 2, 2, rows // 2, 2 * head),
            low(z, 2, rows // 2, 2 * head),
            low(z, rows // 2, 2 * head),
            low(z - 1, rows // 2, 2 * head),
            full(4, 8, width // z),
            full(6, 8, width // z),
            low(6, rows, units),
            low(2, rows, units),
            dma(6 + z),
            dma(2),
            dma(9),
            dma(9),
            dma(3, z),
            dma(3, z),
            dma(3),
            dma(3),
            dma(z),
            dma(z),
            dma(z),
            dma(z + 1),
            dma(2, z, 2),
            dma(2, z, 2),
            dma(2, z),
            dma(2, z),
            dma(2, z),
            dma(2, z + 1),
            dma(2),
            dma(2),
            dma(z),
            dma(z),
            dma(6),
            dma(6),
        ],
        compiler_params=pltpu.CompilerParams(
            collective_id=2, has_side_effects=True, vmem_limit_bytes=VMEM_BYTES
        ),
        cost_estimate=pl.CostEstimate(
            flops=14 * seq * width * cols,
            bytes_accessed=10 * width * cols,
            transcendentals=seq * seq * cols // head,
        ),
    )(
        tokens,
        gains,
        gain_part,
        normed_one,
        rotated,
        keys,
        values,
        attn_vals,
        *table,
        allowed,
        kv_weight.reshape(z, 2, 2, 2, rows // 2, kv_weight.shape[1]),
        query_weight,
        out_weight,
        mix_parts,
        grad_mid,
        grad_mid_low,
        mid,
        ffn_sums,
    )


def layout_kernel(z_size, main, sum_ref, ffn_ref, *refs):
    whole_in, (wg_ref, wu_ref, wd_ref), whole_out, sem = refs[:5], refs[5:8], refs[8:13], refs[13]
    me_z = lax.axis_index("z")
    copies = [
        pltpu.make_async_copy(src, dst, sem.at[index])
        for index, (src, dst) in enumerate(zip(whole_in, whole_out))
    ]

    @pl.when(pl.program_id(0) == 0)
    def _():
        for copy in copies:
            copy.start()

    for kind, out in enumerate((wg_ref, wu_ref, wd_ref)):
        for step in range(z_size):
            at = lax.rem(me_z - step + z_size, z_size)
            values = ffn_ref[kind, step].astype(jnp.float32)
            if step == 0:
                values = values + sum_ref[kind, 0, 0].astype(jnp.float32)
            body = pl.ds(pl.multiple_of(at * main, 128), main)
            out[:, body] = values[:, :main]

            @pl.when((at > 0) & (at < z_size - 1))
            def _(out=out, at=at, values=values):
                tail = z_size * main + lax.rem(at + 1, 2) * 128
                out[:, pl.ds(pl.multiple_of(tail, 128), 128)] = values[:, main:]

    @pl.when(pl.program_id(0) == pl.num_programs(0) - 1)
    def _():
        for copy in copies:
            copy.wait()


def layout_call(ffn_sums, ffn_grads, query_grad, out_grad, kv_grad, mixed, tokens_grad, ffn_cols):
    z_size = lax.axis_size("z")
    main, units = ragged_split(ffn_cols, z_size)
    rows = ffn_grads.shape[2]
    whole = (query_grad, out_grad, kv_grad, mixed, tokens_grad)
    block = rows // 5
    any_ = pl.BlockSpec(memory_space=pl.ANY)
    return pl.pallas_call(
        functools.partial(layout_kernel, z_size, main),
        grid=(5,),
        out_shape=(
            *[jax.ShapeDtypeStruct((rows, ffn_cols), jnp.float32)] * 3,
            *[jax.ShapeDtypeStruct(array.shape, array.dtype) for array in whole],
        ),
        in_specs=[
            pl.BlockSpec((3, 1, 1, block, units), lambda index: (0, 0, 0, index, 0)),
            pl.BlockSpec((3, z_size, block, units), lambda index: (0, 0, index, 0)),
            *[any_] * 5,
        ],
        out_specs=(
            *[pl.BlockSpec((block, ffn_cols), lambda index: (index, 0))] * 3,
            *[any_] * 5,
        ),
        scratch_shapes=[pltpu.SemaphoreType.DMA((5,))],
        compiler_params=pltpu.CompilerParams(vmem_limit_bytes=VMEM_BYTES),
    )(ffn_sums, ffn_grads, *whole)


FF_SPLIT = 4


def ffn_pass(normed, grad_out, gate_weight, up_weight, down_weight):
    gate = jnp.dot(normed, gate_weight, preferred_element_type=jnp.float32)
    up_proj = jnp.dot(normed, up_weight, preferred_element_type=jnp.float32)
    grad_hidden = jnp.dot(grad_out, down_weight, preferred_element_type=jnp.float32)
    product, pull = jax.vjp(gelu_product, gate, up_proj)
    hidden = product.astype(jnp.bfloat16)
    grad_gate_f, grad_up_f = pull(grad_hidden)
    grad_gate = grad_gate_f.astype(jnp.bfloat16)
    grad_up = grad_up_f.astype(jnp.bfloat16)
    mixed_part = matmul_nt(hidden, down_weight).astype(jnp.bfloat16)
    normed_part = (matmul_nt(grad_gate, gate_weight) + matmul_nt(grad_up, up_weight)).astype(
        jnp.bfloat16
    )
    weight_parts = [
        matmul_tn(normed, grad_gate).astype(jnp.bfloat16),
        matmul_tn(normed, grad_up).astype(jnp.bfloat16),
        matmul_tn(grad_out, hidden).astype(jnp.bfloat16),
    ]
    return mixed_part, normed_part, weight_parts


def shards_general(
    tokens,
    segments,
    positions,
    cotangent,
    attn_gain,
    ffn_gain,
    w_kv,
    w_query,
    w_out,
    w_gate,
    w_up,
    w_down,
):
    everywhere = ("z", "xc", "mp")
    dp = ("z", "xc")
    z_size = lax.axis_size("z")
    xc_size = lax.axis_size("xc")
    gains = lax.all_gather(
        jnp.stack([attn_gain, ffn_gain], axis=1), everywhere, axis=0, tiled=True
    ).astype(jnp.float32)
    gain_one, gain_two = gains[:, 0], gains[:, 1]
    kv_weight = lax.all_gather(w_kv, everywhere, axis=0, tiled=True)
    head_dim = kv_weight.shape[1] // 2
    width = tokens.shape[1]
    seq_len = segments.shape[0]
    heads_here = w_query.shape[1] // head_dim
    scale = head_dim ** (-0.5)
    cosine, sine = rotary_angles(positions, head_dim)
    inputs_f = tokens.astype(jnp.float32)
    tokens_all = lax.all_gather(tokens, "mp", axis=0, tiled=True)
    normed_one = norm_gain(tokens_all.astype(jnp.float32), gain_one).astype(jnp.bfloat16)
    query_weight = lax.all_gather(w_query, dp, axis=0, tiled=True)
    out_weight = lax.all_gather(w_out, dp, axis=0, tiled=True)

    rows = w_gate.shape[0]
    unit = w_gate.shape[1] // z_size

    def spread(weight):
        pieces = weight.reshape(rows, z_size, unit).transpose(1, 0, 2)
        pieces = lax.all_to_all(pieces, "z", split_axis=0, concat_axis=0, tiled=True)
        return lax.all_gather(pieces, "xc", axis=1, tiled=False).reshape(width, unit)

    gate_weight, up_weight, down_weight = spread(w_gate), spread(w_up), spread(w_down)
    grad_all = lax.all_gather(cotangent, ("z", "mp"), axis=0, tiled=True)

    query = jnp.dot(normed_one, query_weight, preferred_element_type=jnp.float32).reshape(
        seq_len, heads_here, head_dim
    )
    rotated = (rotate(query, cosine[:, None], sine[:, None]) * scale).astype(jnp.bfloat16)
    keyval = jnp.dot(normed_one, kv_weight, preferred_element_type=jnp.float32)
    keys = rotate(keyval[:, :head_dim], cosine, sine).astype(jnp.bfloat16)
    values = keyval[:, head_dim:].astype(jnp.bfloat16)
    allowed = block_allowed(segments, 0, seq_len)
    scores = jnp.einsum("thd,sd->hts", rotated, keys, preferred_element_type=jnp.float32)
    scores = jnp.where(allowed[None], scores, masked_score)
    row_max = jnp.max(scores, axis=-1, keepdims=True)
    weights = jnp.exp(scores - row_max)
    probs = weights / jnp.sum(weights, axis=-1, keepdims=True)
    probs_low = probs.astype(jnp.bfloat16)
    attn_vals = (
        jnp.einsum("hts,sd->thd", probs_low, values, preferred_element_type=jnp.float32)
        .reshape(seq_len, heads_here * head_dim)
        .astype(jnp.bfloat16)
    )
    mid = inputs_f + lax.psum_scatter(
        matmul_nt(attn_vals, out_weight).astype(jnp.bfloat16),
        "mp",
        scatter_dimension=0,
        tiled=True,
    ).astype(jnp.float32)
    normed_two = norm_gain(mid, gain_two).astype(jnp.bfloat16)
    normed_all = lax.all_gather(normed_two, ("z", "mp"), axis=0, tiled=True)

    mixed_part, normed_part, weight_parts = ffn_pass(
        normed_all, grad_all, gate_weight, up_weight, down_weight
    )
    grad_normed_two = lax.psum_scatter(
        normed_part, ("z", "mp"), scatter_dimension=0, tiled=True
    ).astype(jnp.float32)
    mixed = (
        mid
        + lax.psum_scatter(mixed_part, ("z", "mp"), scatter_dimension=0, tiled=True).astype(
            jnp.float32
        )
    ).astype(jnp.bfloat16)

    def collect(part):
        pieces = part.reshape(z_size, xc_size, rows, unit).transpose(1, 0, 2, 3)
        pieces = pieces.reshape(xc_size * z_size * rows, unit)
        pieces = lax.psum_scatter(pieces, "xc", scatter_dimension=0, tiled=True)
        pieces = pieces.reshape(z_size, rows, unit)
        pieces = lax.all_to_all(pieces, "z", split_axis=0, concat_axis=0, tiled=True)
        return pieces.transpose(1, 0, 2).reshape(rows, z_size * unit).astype(jnp.float32)

    w_gate_grad, w_up_grad, w_down_grad = [collect(part) for part in weight_parts]

    norm_pull_two = jax.vjp(norm_gain, mid, gain_two)[1]
    grad_mid_norm, grad_gain_two = norm_pull_two(grad_normed_two)
    grad_mid = cotangent.astype(jnp.float32) + grad_mid_norm
    grad_mid_all = lax.all_gather(grad_mid.astype(jnp.bfloat16), "mp", axis=0, tiled=True)
    grad_vals = (
        jnp.dot(grad_mid_all, out_weight, preferred_element_type=jnp.float32)
        .astype(jnp.bfloat16)
        .reshape(seq_len, heads_here, head_dim)
    )
    grad_probs = jnp.einsum("thd,sd->hts", grad_vals, values, preferred_element_type=jnp.float32)
    delta = jnp.sum(probs * grad_probs, axis=-1, keepdims=True)
    grad_scores = (probs * (grad_probs - delta)).astype(jnp.bfloat16)
    grad_rot = jnp.einsum("hts,sd->thd", grad_scores, keys, preferred_element_type=jnp.float32)
    key_sum = jnp.einsum("hts,thd->sd", grad_scores, rotated, preferred_element_type=jnp.float32)
    value_sum = jnp.einsum("hts,thd->sd", probs_low, grad_vals, preferred_element_type=jnp.float32)
    grad_query = (
        (unrotate(grad_rot, cosine[:, None], sine[:, None]) * scale)
        .reshape(seq_len, heads_here * head_dim)
        .astype(jnp.bfloat16)
    )
    grad_kv = jnp.concatenate([unrotate(key_sum, cosine, sine), value_sum], axis=1).astype(
        jnp.bfloat16
    )
    grad_normed_one = lax.psum_scatter(
        (matmul_nt(grad_query, query_weight) + matmul_nt(grad_kv, kv_weight)).astype(jnp.bfloat16),
        "mp",
        scatter_dimension=0,
        tiled=True,
    ).astype(jnp.float32)
    norm_pull_one = jax.vjp(norm_gain, inputs_f, gain_one)[1]
    grad_input_norm, grad_gain_one = norm_pull_one(grad_normed_one)
    tokens_grad = (grad_mid + grad_input_norm).astype(jnp.bfloat16)

    w_query_grad = lax.psum_scatter(
        matmul_tn(normed_one, grad_query).astype(jnp.bfloat16), dp, scatter_dimension=0, tiled=True
    ).astype(jnp.float32)
    w_out_grad = lax.psum_scatter(
        matmul_tn(grad_mid_all, attn_vals).astype(jnp.bfloat16), dp, scatter_dimension=0, tiled=True
    ).astype(jnp.float32)
    small = jnp.concatenate(
        [matmul_tn(normed_one, grad_kv), grad_gain_one[:, None], grad_gain_two[:, None]], axis=1
    )
    small = lax.psum_scatter(small, everywhere, scatter_dimension=0, tiled=True)
    kv_grad = small[:, : 2 * head_dim]
    return (
        mixed,
        tokens_grad,
        small[:, 2 * head_dim],
        small[:, 2 * head_dim + 1],
        kv_grad,
        w_query_grad,
        w_out_grad,
        w_gate_grad,
        w_up_grad,
        w_down_grad,
    )


def shards_fast(
    tokens,
    segments,
    positions,
    cotangent,
    attn_gain,
    ffn_gain,
    w_kv,
    w_query,
    w_out,
    w_gate,
    w_up,
    w_down,
):
    quarter = w_kv.shape[1] // 8
    lane = jnp.arange(2 * quarter)
    freqs = rope_base ** (-(lane % quarter).astype(jnp.float32) / quarter)
    phase = positions.astype(jnp.float32)[:, None] * freqs[None, :]
    table = (jnp.cos(phase), jnp.where(lane < quarter, -1.0, 1.0)[None, :] * jnp.sin(phase))
    (
        normed_one,
        rotated,
        keys,
        values,
        attn_vals,
        mid,
        normed_two,
        gains,
        allowed,
        kv_weight,
        query_weight,
        out_weight,
        ffn_weights,
        grad_all,
    ) = pre_call(
        tokens,
        w_kv,
        attn_gain[None, :],
        ffn_gain[None, :],
        table,
        segments[None, :],
        cotangent,
        w_query,
        w_out,
        (w_gate, w_up, w_down),
    )
    main = ragged_split(w_gate.shape[1], lax.axis_size("z"))[0]
    grad_mid, gain_part, mix_parts, ffn_sums, grad_mid_low = ffn_call(
        gains, normed_two, grad_all, ffn_weights, mid, w_gate.shape[0], main
    )
    mixed, tokens_grad, gain_grads, kv_grad, query_grad, out_grad, ffn_grads = post_call(
        tokens,
        gains,
        gain_part,
        normed_one,
        rotated,
        keys,
        values,
        attn_vals,
        table,
        allowed,
        kv_weight,
        query_weight,
        out_weight,
        mix_parts,
        grad_mid,
        grad_mid_low,
        mid,
        ffn_sums,
        main,
    )
    *ffn_out, query_grad, out_grad, kv_grad, mixed, tokens_grad = layout_call(
        ffn_sums,
        ffn_grads,
        query_grad,
        out_grad,
        kv_grad,
        mixed,
        tokens_grad,
        w_gate.shape[1],
    )
    share = attn_gain.shape[0]
    place = lax.axis_index(("z", "x", "c", "mp")) * share
    gain_grads = gain_grads.reshape(2, gain_grads.size // 2)
    gain_grads = lax.dynamic_slice(gain_grads, (0, place), (2, share))
    return (
        mixed,
        tokens_grad,
        gain_grads[0],
        gain_grads[1],
        kv_grad,
        query_grad,
        out_grad,
        *ffn_out,
    )


def solution(mesh):
    dp_size, mp_size = mesh.shape["dp"], mesh.shape["mp"]
    if dp_size == 4 * FF_SPLIT and mp_size == 2:
        body, dp = shards_fast, ("z", "x", "c")
        sizes = (FF_SPLIT, 2, 2, mp_size)
    else:
        body, dp = shards_general, ("z", "xc")
        sizes = (FF_SPLIT, dp_size // FF_SPLIT, mp_size)
    all_axes = (*dp, "mp")
    fine = jax.sharding.Mesh(mesh.devices.reshape(sizes), all_axes)
    in_specs = (
        P(all_axes, None),
        P(dp),
        P(dp),
        P(all_axes, None),
        P(all_axes),
        P(all_axes),
        P(all_axes, None),
        P(dp, "mp"),
        P(dp, "mp"),
        P(dp, "mp"),
        P(dp, "mp"),
        P(dp, "mp"),
    )
    out_specs = (
        P(all_axes, None),
        P(all_axes, None),
        P(all_axes),
        P(all_axes),
        P(all_axes, None),
        P(dp, "mp"),
        P(dp, "mp"),
        P(dp, "mp"),
        P(dp, "mp"),
        P(dp, "mp"),
    )
    return jax.shard_map(body, mesh=fine, in_specs=in_specs, out_specs=out_specs, check_vma=False)
```

```python
import functools

import jax
import jax.numpy as jnp
from jax import lax
from jax.experimental import pallas as pl
from jax.experimental.pallas import tpu as pltpu
from jax.sharding import PartitionSpec as P

WINDOW = 2048


epsilon = 1e-06
rope_base = 10000.0
masked_score = -1e30
VMEM_BYTES = 66_000_000


def norm_gain(values, gain):
    return values * lax.rsqrt(jnp.mean(values * values, axis=-1, keepdims=True) + epsilon) * gain


def rotary_angles(positions, head_width):
    quarter = head_width // 4
    freqs = rope_base ** (-jnp.arange(quarter).astype(jnp.float32) / quarter)
    phase = positions.astype(jnp.float32)[:, None] * freqs[None, :]
    return (jnp.cos(phase), jnp.sin(phase))


def rotate(values, cosine, sine):
    quarter = cosine.shape[-1]
    first_half = values[..., :quarter]
    second_half = values[..., quarter : 2 * quarter]
    return jnp.concatenate(
        [
            first_half * cosine - second_half * sine,
            second_half * cosine + first_half * sine,
            values[..., 2 * quarter :],
        ],
        axis=-1,
    )


def unrotate(values, cosine, sine):
    quarter = cosine.shape[-1]
    first_half = values[..., :quarter]
    second_half = values[..., quarter : 2 * quarter]
    return jnp.concatenate(
        [
            first_half * cosine + second_half * sine,
            second_half * cosine - first_half * sine,
            values[..., 2 * quarter :],
        ],
        axis=-1,
    )


def gelu_product(gate, up_proj):
    return jax.nn.gelu(gate, approximate=True) * up_proj


def matmul_nt(left, right):
    return lax.dot_general(
        left, right, (((1,), (1,)), ((), ())), preferred_element_type=jnp.float32
    )


def matmul_tn(left, right):
    return lax.dot_general(
        left, right, (((0,), (0,)), ((), ())), preferred_element_type=jnp.float32
    )


def block_allowed(segments, first_row, rows):
    seq_len = segments.shape[0]
    query_rows = first_row + jnp.arange(rows)
    key_rows = jnp.arange(seq_len)
    return (
        (segments[:, None] == segments[None, :])
        & (key_rows[None, :] <= query_rows[:, None])
        & (query_rows[:, None] - key_rows[None, :] < WINDOW)
    )


MESH_ID = pl.DeviceIdType.MESH
GELU_A = 0.7978845608028654
GELU_B = 0.044715
TILE = 256
WIDE = 512


def remote(src, dst, send_sem, recv_sem, where):
    return pltpu.make_async_remote_copy(
        src_ref=src,
        dst_ref=dst,
        send_sem=send_sem,
        recv_sem=recv_sem,
        device_id=where,
        device_id_type=MESH_ID,
    )


class Halves:
    def __init__(self, src, dst, send_sem, recv_sem, where):
        rows = src.shape[0] // 2
        cuts = [pl.ds(part * rows, rows) for part in range(2)]
        self.copies = [
            remote(src.at[cut], dst.at[cut], send_sem.at[part], recv_sem.at[part], where)
            for part, cut in enumerate(cuts)
        ]

    def start(self):
        for copy in self.copies:
            copy.start()

    def wait_recv(self):
        for copy in self.copies:
            copy.wait_recv()

    def wait_send(self):
        for copy in self.copies:
            copy.wait_send()


def dot_nn(left, right):
    return lax.dot_general(
        left, right, (((1,), (0,)), ((), ())), preferred_element_type=jnp.float32
    )


def gelu_parts(gate):
    square = gate * gate
    bend = jnp.tanh(GELU_A * gate * (1.0 + GELU_B * square))
    half = 0.5 * (1.0 + bend)
    slope = half + 0.5 * gate * (1.0 - bend * bend) * GELU_A * (1.0 + 3.0 * GELU_B * square)
    return gate * half, slope


def add_rows(first, rest, out, count):
    def body(index, carry):
        step = pl.ds(pl.multiple_of(index * 32, 32), 32)
        total = first[step, :].astype(jnp.float32)
        for other in rest:
            total = total + other[step, :].astype(jnp.float32)
        out[step, :] = total.astype(out.dtype)
        return carry

    lax.fori_loop(0, count // 32, body, 0)


def norm_back(values, gain, upstream):
    scale = lax.rsqrt(jnp.mean(values * values, axis=-1, keepdims=True) + epsilon)
    normed = values * scale
    pulled = gain * upstream
    back = scale * (pulled - normed * jnp.mean(normed * pulled, axis=-1, keepdims=True))
    return back, jnp.sum(upstream * normed, axis=0, keepdims=True)


def ffn_kernel(
    z_size,
    main,
    gain_ref,
    own_hbm,
    dy_hbm,
    w_hbm,
    mid_hbm,
    gm_ref,
    gain_part,
    mix_hbm,
    sums_hbm,
    gm_hbm,
    n2,
    dy,
    w3,
    h3,
    n2_t,
    dy_t,
    gn_part,
    mix_buf,
    gn_y,
    gn_z,
    gn_s,
    c_in,
    x_in,
    mid,
    load_sem,
    mix_sem,
    ag_y_send,
    ag_y_recv,
    ag_z_send,
    ag_z_recv,
    rs_y_send,
    rs_y_recv,
    rs_z_send,
    rs_z_recv,
    c_send,
    c_recv,
    x_send,
    x_recv,
    out_sem,
):
    own = own_hbm.shape[0] // 2
    width = own_hbm.shape[1]
    units = w3.shape[2]
    rows = c_in.shape[3]
    span = width // z_size
    me_y, me_z = lax.axis_index("mp"), lax.axis_index("z")
    me_x, me_c = lax.axis_index("x"), lax.axis_index("c")
    mine = pl.ds(pl.multiple_of(me_y * own, own), own)
    theirs = pl.ds(pl.multiple_of((1 - me_y) * own, own), own)
    to_y, to_x, to_c = {"mp": 1 - me_y}, {"x": 1 - me_x}, {"c": 1 - me_c}

    def ahead(step):
        return lax.rem(me_z + step, z_size)

    def to_z(step):
        return {"z": ahead(step)}

    def row_block(z_at, x_at, c_at):
        return pl.ds(pl.multiple_of(((z_at * 2 + x_at) * 2 + c_at) * rows, rows), rows)

    inner = (me_z > 0) & (me_z < z_size - 1)
    outer = (me_z == 0) | (me_z == z_size - 1)

    def w_load(index, columns):
        cols = pl.ds(0, columns)
        return pltpu.make_async_copy(
            w_hbm.at[index, :, cols], w3.at[index, :, cols], load_sem.at[z_size + index]
        )

    def w_loads(act):
        for case, columns in ((inner, units), (outer, main)):

            @pl.when(case)
            def _(columns=columns):
                for index in range(3):
                    act(w_load(index, columns))

    w_loads(lambda copy: copy.start())
    dy_loads = [
        pltpu.make_async_copy(dy_hbm.at[index], dy, load_sem.at[index])
        for index in range(z_size)
    ]
    own_load = pltpu.make_async_copy(own_hbm, n2.at[0], load_sem.at[z_size + 3])
    mid_load = pltpu.make_async_copy(mid_hbm, mid, load_sem.at[z_size + 4])
    for load in (own_load, dy_loads[0], mid_load):
        load.start()

    barrier = pltpu.get_barrier_semaphore()
    peers = [to_y, to_x, to_c] + [to_z(step) for step in range(1, z_size)]
    for where in peers:
        pl.semaphore_signal(barrier, inc=1, device_id=where, device_id_type=MESH_ID)
    pl.semaphore_wait(barrier, len(peers))

    def ag_y(index):
        block = n2.at[index, mine]
        return Halves(block, block, ag_y_send.at[index], ag_y_recv.at[index], to_y)

    def ag_y_in(index):
        block = n2.at[index, theirs]
        return Halves(block, block, ag_y_send.at[index], ag_y_recv.at[index], to_y)

    def ag_z(index):
        src = own_hbm.at[mine] if index == 0 else n2.at[index, mine]
        return Halves(
            src, n2.at[index + 1, mine], ag_z_send.at[index], ag_z_recv.at[index + 1], to_z(1)
        )

    def ag_z_in(index):
        block = n2.at[index, mine]
        return Halves(block, block, ag_z_send.at[0], ag_z_recv.at[index], to_z(1))

    def ag_last():
        return Halves(
            n2.at[2, theirs], n2.at[3, theirs], ag_y_send.at[3], ag_y_recv.at[3], to_z(1)
        )

    def forward(index):
        ag_z_in(index).wait_recv()
        ag_z(index).start()
        ag_y(index).start()

    ag_z(0).start()

    mix_copies = []

    def turn(source, target, index):
        def turn_tile(tile, carry):
            at = pl.ds(pl.multiple_of(tile * span, 128), span)
            target[at, pl.ds(index * 2 * own, 2 * own)] = source[:, at].T
            return carry

        lax.fori_loop(0, z_size, turn_tile, 0)

    def chunk(index):
        if index:
            mix_copies[index - 1].wait()
        dy_loads[index].wait()
        rows_at = pl.ds(index * 2 * own, 2 * own)

        def up_tile(tile, carry):
            cols = pl.ds(pl.multiple_of(tile * WIDE, WIDE), WIDE)
            gate = dot_nn(n2[index], w3[0, :, cols])
            up_proj = dot_nn(n2[index], w3[1, :, cols])
            grad_hidden = dot_nn(dy[...], w3[2, :, cols])
            act, slope = gelu_parts(gate)
            h3[0, rows_at, cols] = (grad_hidden * up_proj * slope).astype(jnp.bfloat16)
            h3[1, rows_at, cols] = (grad_hidden * act).astype(jnp.bfloat16)
            h3[2, rows_at, cols] = (act * up_proj).astype(jnp.bfloat16)
            return carry

        lax.fori_loop(0, units // WIDE, up_tile, 0)

        def down_tile(tile, carry):
            at = pl.ds(pl.multiple_of(tile * span, 128), span)
            normed = matmul_nt(w3[0, at, :], h3[0, rows_at, :]) + matmul_nt(
                w3[1, at, :], h3[1, rows_at, :]
            )
            mixed = matmul_nt(w3[2, at, :], h3[2, rows_at, :])
            for half in range(2):
                cols = slice(half * own, (half + 1) * own)
                gn_part[index, half, at, :] = normed[:, cols].astype(jnp.bfloat16)
                mix_buf[half, at, :] = mixed[:, cols].astype(jnp.bfloat16)
            return carry

        lax.fori_loop(0, z_size, down_tile, 0)
        copy = pltpu.make_async_copy(mix_buf, mix_hbm.at[index], mix_sem.at[index])
        copy.start()
        mix_copies.append(copy)
        if index:
            rs_y(index).start()
        turn(n2.at[index], n2_t, index)
        turn(dy, dy_t, index)
        if index + 1 < z_size:
            dy_loads[index + 1].start()

    def rs_y(index):
        return Halves(
            gn_part.at[index, 1 - me_y], gn_y.at[index], rs_y_send.at[index], rs_y_recv.at[index], to_y
        )

    def rs_z(index):
        return Halves(
            gn_s.at[index - 1],
            gn_z.at[index - 1],
            rs_z_send.at[index],
            rs_z_recv.at[index - 1],
            to_z(1),
        )

    def rs_step(index):
        rs_y(index).wait_recv()
        slot = (index - 2) % z_size
        if index != 1:
            Halves(
                gn_s.at[slot], gn_z.at[slot], rs_z_send.at[1], rs_z_recv.at[slot], to_z(1)
            ).wait_recv()

        def add_tile(tile, carry):
            at = pl.ds(pl.multiple_of(tile * TILE, TILE), TILE)
            total = gn_part[index, me_y, at, :].astype(jnp.float32) + gn_y[index, at, :].astype(
                jnp.float32
            )
            if index != 1:
                total = total + gn_z[slot, at, :].astype(jnp.float32)
            if index == 0:
                gm_ref[:, at] = total.T
            else:
                gn_s[index - 1, at, :] = total.astype(jnp.bfloat16)
            return carry

        lax.fori_loop(0, width // TILE, add_tile, 0)
        if index != 0:
            rs_z(index).start()


    def grads(step):
        at = pl.ds(pl.multiple_of(ahead(step) * span, 128), span)
        for kind, source in enumerate((n2_t, n2_t, dy_t)):

            def tile_body(tile, carry, kind=kind, source=source):
                cols = pl.ds(pl.multiple_of(tile * WIDE, WIDE), WIDE)
                w3[kind, at, cols] = dot_nn(source[at, :], h3[kind, :, cols]).astype(jnp.bfloat16)
                return carry

            lax.fori_loop(0, units // WIDE, tile_body, 0)
            for far in (1, 0):
                over_c(kind, step, far).start()

    def over_c(kind, step, far):
        x_at = 1 - me_x if far else me_x
        return remote(
            w3.at[kind, row_block(ahead(step), x_at, 1 - me_c)],
            c_in.at[kind, step, far],
            c_send.at[kind, step, far],
            c_recv.at[kind, step, far],
            to_c,
        )

    def over_x(kind):
        return remote(
            w3.at[kind, row_block(ahead(1), 1 - me_x, me_c)],
            x_in.at[kind],
            x_send.at[kind],
            x_recv.at[kind],
            to_x,
        )

    out_copies = []

    def keep(kind, step, far, block):
        copy = pltpu.make_async_copy(
            block, sums_hbm.at[kind, step, far], out_sem.at[kind, step, far]
        )
        copy.start()
        out_copies.append(copy)

    def core_sums(step):
        pairs = [(kind, far) for kind in range(3) for far in (1, 0)]
        if step == 1:
            pairs.sort(key=lambda pair: -pair[1])
        for kind, far in pairs:
            over_c(kind, step, far).wait_recv()
            x_at = 1 - me_x if far else me_x
            block = w3.at[kind, row_block(ahead(step), x_at, me_c)]
            add_rows(block, [c_in.at[kind, step, far]], block, rows)
            if step != 1:
                keep(kind, step, far, block)
            elif far:
                over_x(kind).start()

    def first_sums():
        for kind in range(3):
            over_x(kind).wait_recv()
            block = w3.at[kind, row_block(ahead(1), me_x, me_c)]
            add_rows(block, [x_in.at[kind]], block, rows)
            keep(kind, 1, 0, block)

    own_load.wait()
    w_loads(lambda copy: copy.wait())

    @pl.when(outer)
    def _():
        w3[:, :, main:] = jnp.zeros((3, width, units - main), jnp.bfloat16)

    chunk(0)
    forward(1)
    forward(2)
    ag_y_in(1).wait_recv()
    chunk(1)
    ag_y_in(2).wait_recv()
    ag_last().start()
    chunk(2)
    rs_step(1)
    ag_z_in(3).wait_recv()
    ag_last().wait_recv()
    chunk(3)
    rs_y(0).start()
    rs_step(2)
    grads(1)
    grads(2)
    core_sums(1)
    rs_step(3)
    grads(3)
    core_sums(2)
    grads(0)
    core_sums(3)
    rs_step(0)
    core_sums(0)

    cot_load = pltpu.make_async_copy(
        dy_hbm.at[0, mine], dy.at[pl.ds(0, own)], load_sem.at[z_size + 3]
    )
    cot_load.start()
    cot_load.wait()
    mid_load.wait()

    def mid_rows(index, total):
        at = pl.ds(pl.multiple_of(index * 32, 32), 32)
        grad, gain_sum = norm_back(mid[at, :], gain_ref[1:2, :], gm_ref[at, :])
        grad = grad + dy[at, :].astype(jnp.float32)
        gm_ref[at, :] = grad
        dy[pl.ds(pl.multiple_of(own + index * 32, 32), 32), :] = grad.astype(jnp.bfloat16)
        return total + gain_sum

    gain_sum = lax.fori_loop(0, own // 32, mid_rows, jnp.zeros((1, width), jnp.float32))
    gm_save = pltpu.make_async_copy(dy.at[pl.ds(own, own)], gm_hbm, load_sem.at[z_size + 3])
    gm_save.start()
    for index in range(4):
        gain_part[index : index + 1, :] = jnp.zeros((1, span), jnp.float32)
        gain_part[4 + index : 5 + index, :] = gain_sum[:, index * span : (index + 1) * span]
    first_sums()
    gm_save.wait()

    for copy in mix_copies[3:] + out_copies:
        copy.wait()
    for index in range(z_size):
        if index in (1, 2):
            ag_y(index).wait_send()
        if index == 3:
            ag_last().wait_send()
        rs_y(index).wait_send()
        if index < z_size - 1:
            ag_z(index).wait_send()
        if index:
            rs_z(index).wait_send()
        for kind in range(3):
            over_c(kind, index, 0).wait_send()
            over_c(kind, index, 1).wait_send()
            if index == 1:
                over_x(kind).wait_send()


def ffn_call(gains, normed, grad_all, weights, mid, rows, main):
    z_size = lax.axis_size("z")
    pair, width = normed.shape
    units = weights.shape[2]
    own = pair // 2
    wide = lambda *lead: pltpu.VMEM((*lead, width), jnp.bfloat16)
    tall = lambda *lead: pltpu.VMEM((*lead, width, own), jnp.bfloat16)
    dma = lambda *lead: pltpu.SemaphoreType.DMA(lead)
    vmem = pl.BlockSpec(memory_space=pltpu.VMEM)
    hbm = pl.BlockSpec(memory_space=pl.ANY)
    return pl.pallas_call(
        functools.partial(ffn_kernel, z_size, main),
        out_shape=(
            jax.ShapeDtypeStruct((own, width), jnp.float32),
            jax.ShapeDtypeStruct((8, width // z_size), jnp.float32),
            jax.ShapeDtypeStruct((z_size, 2, width, own), jnp.bfloat16),
            jax.ShapeDtypeStruct((3, z_size, 2, rows, units), jnp.bfloat16),
            jax.ShapeDtypeStruct((own, width), jnp.bfloat16),
        ),
        in_specs=[vmem, hbm, hbm, hbm, hbm],
        out_specs=(vmem, vmem, hbm, hbm, hbm),
        scratch_shapes=[
            wide(z_size, pair),
            wide(pair),
            pltpu.VMEM(weights.shape, jnp.bfloat16),
            pltpu.VMEM((3, z_size * pair, units), jnp.bfloat16),
            pltpu.VMEM((width, z_size * pair), jnp.bfloat16),
            pltpu.VMEM((width, z_size * pair), jnp.bfloat16),
            tall(z_size, 2),
            tall(2),
            tall(z_size),
            tall(z_size - 1),
            tall(z_size - 1),
            pltpu.VMEM((3, z_size, 2, rows, units), jnp.bfloat16),
            pltpu.VMEM((3, rows, units), jnp.bfloat16),
            pltpu.VMEM((own, width), jnp.float32),
            dma(z_size + 5),
            dma(z_size),
            dma(z_size, 2),
            dma(z_size, 2),
            dma(z_size, 2),
            dma(z_size, 2),
            dma(z_size, 2),
            dma(z_size, 2),
            dma(z_size, 2),
            dma(z_size, 2),
            dma(3, z_size, 2),
            dma(3, z_size, 2),
            dma(3),
            dma(3),
            dma(3, z_size, 2),
        ],
        compiler_params=pltpu.CompilerParams(
            collective_id=0, has_side_effects=True, vmem_limit_bytes=VMEM_BYTES
        ),
        cost_estimate=pl.CostEstimate(
            flops=18 * z_size * pair * width * units,
            bytes_accessed=4 * weights.size + 12 * z_size * pair * width,
            transcendentals=z_size * pair * units,
        ),
    )(gains, normed, grad_all, weights, mid)


def spin(values, table):
    first = values[:, : values.shape[1] // 2]
    turned = first * table[0] + pltpu.roll(first, first.shape[1] // 2, 1) * table[1]
    return jnp.concatenate([turned, values[:, values.shape[1] // 2 :]], axis=1)


def spin_back(values, table):
    first = values[:, : values.shape[1] // 2]
    turned = first * table[0] - pltpu.roll(first, first.shape[1] // 2, 1) * table[1]
    return jnp.concatenate([turned, values[:, values.shape[1] // 2 :]], axis=1)


def head_probs(rotated, keys, allowed):
    scores = jnp.where(allowed > 0.5, matmul_nt(rotated, keys), masked_score)
    weights = jnp.exp(scores - jnp.max(scores, axis=-1, keepdims=True))
    return weights / jnp.sum(weights, axis=-1, keepdims=True)


def ragged_split(columns, parts):
    main = columns // parts // 128 * 128
    return main, main + 128


def pre_kernel(
    z_size,
    tok_ref,
    wkv_ref,
    gain_one_ref,
    gain_two_ref,
    cos_ref,
    sin_ref,
    seg_ref,
    cot_hbm,
    wq_hbm,
    wo_hbm,
    wg_hbm,
    wu_hbm,
    wd_hbm,
    n1_ref,
    rot_ref,
    key_ref,
    val_ref,
    att_ref,
    mid_ref,
    n2_ref,
    gain_ref,
    allow_ref,
    kv_out,
    wq_out,
    wo_out,
    w3_save,
    dy_save,
    w3_out,
    dy_out,
    kv_w,
    q_w,
    o_w,
    tok,
    part,
    part_y,
    query,
    gain_rows,
    y_send,
    y_recv,
    ky_send,
    ky_recv,
    az_send,
    az_recv,
    ax_send,
    ax_recv,
    ac_send,
    ac_recv,
    fz_send,
    fz_recv,
    fx_send,
    fx_recv,
    fc_send,
    fc_recv,
    dz_send,
    dz_recv,
    dy_send,
    dy_recv,
    local_sem,
):
    me_z, me_x = lax.axis_index("z"), lax.axis_index("x")
    me_c, me_y = lax.axis_index("c"), lax.axis_index("mp")
    own, width = tok_ref.shape
    rows = wq_hbm.shape[0]
    half_rows = wkv_ref.shape[0]
    head = key_ref.shape[1]
    main, units = ragged_split(wg_hbm.shape[1], z_size)
    to_y, to_x, to_c = {"mp": 1 - me_y}, {"x": 1 - me_x}, {"c": 1 - me_c}

    def to_z(step):
        return {"z": lax.rem(me_z + step, z_size)}

    def from_z(step):
        return lax.rem(me_z - step + z_size, z_size)

    def row_block(step, x_at, c_at):
        start = ((from_z(step) * 2 + x_at) * 2 + c_at) * rows
        return pl.ds(pl.multiple_of(start, rows), rows)

    mine = pl.ds(pl.multiple_of(me_y * own, own), own)
    theirs = pl.ds(pl.multiple_of((1 - me_y) * own, own), own)
    bufs = (kv_w, q_w, o_w)
    inputs = (None, wq_hbm, wo_hbm)

    locals_ = []

    def local(src, dst):
        copy = pltpu.make_async_copy(src, dst, local_sem.at[len(locals_)])
        copy.start()
        locals_.append(copy)
        return copy

    here = row_block(0, me_x, me_c)
    own_q = local(wq_hbm, q_w.at[here])
    own_o = local(wo_hbm, o_w.at[here])
    ffn_in = (wg_hbm, wu_hbm, wd_hbm)

    def body_of(target):
        return pl.ds(pl.multiple_of(target * main, 128), main), pl.ds(0, main)

    def tail_of(target):
        start = z_size * main + lax.rem(target + 1, 2) * 128
        return pl.ds(pl.multiple_of(start, 128), 128), pl.ds(main, 128)

    def is_inner(at):
        return (at > 0) & (at < z_size - 1)

    own_f = []
    for kind in range(3):
        src, dst = body_of(me_z)
        own_f.append(local(ffn_in[kind].at[:, src], w3_out.at[kind, here, dst]))

    def own_tail(kind):
        src, dst = tail_of(me_z)
        return pltpu.make_async_copy(
            ffn_in[kind].at[:, src], w3_out.at[kind, here, dst], local_sem.at[20 + kind]
        )

    @pl.when(is_inner(me_z))
    def _():
        for kind in range(3):
            own_tail(kind).start()
    own_d = local(cot_hbm, dy_out.at[0, mine])

    kv_own = pl.ds(pl.multiple_of(here.start + me_y * half_rows, half_rows), half_rows)
    gain_rows[...] = jnp.zeros(gain_rows.shape, jnp.float32)
    gain_rows[0:1, :half_rows] = gain_one_ref[...].astype(jnp.float32)
    gain_rows[1:2, :half_rows] = gain_two_ref[...].astype(jnp.float32)
    spread = gain_rows[...].T
    kv_w[kv_own, : 2 * head] = wkv_ref[...]
    kv_w[kv_own, 2 * head :] = spread[:half_rows, :].astype(jnp.bfloat16)

    barrier = pltpu.get_barrier_semaphore()
    peers = [to_y, to_x, to_c] + [to_z(step) for step in range(1, z_size)]
    for where in peers:
        pl.semaphore_signal(barrier, inc=1, device_id=where, device_id_type=MESH_ID)
    pl.semaphore_wait(barrier, len(peers))

    tok_y = remote(tok_ref, tok.at[mine], y_send.at[1], y_recv.at[1], to_y)
    tok_y_in = remote(tok_ref, tok.at[theirs], y_send.at[1], y_recv.at[1], to_y)
    part_out = remote(part.at[theirs], part_y, y_send.at[2], y_recv.at[2], to_y)
    n2_y = remote(n2_ref.at[mine], n2_ref.at[mine], y_send.at[3], y_recv.at[3], to_y)
    n2_y_in = remote(n2_ref.at[theirs], n2_ref.at[theirs], y_send.at[3], y_recv.at[3], to_y)

    def block_of(kind, step, x_at):
        if kind:
            return row_block(step, x_at, me_c)
        return kv_rows(step, x_at, me_y)

    def kv_rows(step, x_at, y_at):
        start = row_block(step, x_at, me_c).start + y_at * half_rows
        return pl.ds(pl.multiple_of(start, half_rows), half_rows)

    def kv_y(step, far):
        x_at = 1 - me_x if far else me_x
        block = kv_w.at[kv_rows(step, x_at, me_y)]
        slot = step + z_size * far
        return remote(block, block, ky_send.at[slot], ky_recv.at[slot], to_y)

    def kv_y_in(step, far):
        x_at = 1 - me_x if far else me_x
        block = kv_w.at[kv_rows(step, x_at, 1 - me_y)]
        slot = step + z_size * far
        return remote(block, block, ky_send.at[slot], ky_recv.at[slot], to_y)

    def source(kind, step):
        if isinstance(step, int) and step == 0 and kind:
            return inputs[kind]
        return bufs[kind].at[block_of(kind, step, me_x)]

    first_z, last_z = (z_size - 1 - me_z) // (z_size - 1), me_z // (z_size - 1)
    inner = first_z + last_z == 0
    order = (0, 1 + 2 * first_z, 3 - first_z - last_z, 2 - first_z + last_z)
    hops = (
        None,
        (lax.rem(me_z + 1, z_size), 2),
        (lax.rem(me_z + z_size - 1, z_size), 2),
        (lax.rem(3 * (me_z + 3), z_size), lax.rem(2 * me_z + 3, z_size)),
    )

    def a_z_own(kind, right):
        return remote(
            source(kind, 0),
            bufs[kind].at[block_of(kind, 0, me_x)],
            az_send.at[kind, right],
            az_recv.at[kind, 1 if right else z_size - 1],
            to_z(1 if right else z_size - 1),
        )

    def a_z_start(kind):
        @pl.when(last_z == 0)
        def _():
            a_z_own(kind, 1).start()

        @pl.when(first_z == 0)
        def _():
            a_z_own(kind, 0).start()

    def a_z(kind, index):
        target, slot = hops[index]
        block = bufs[kind].at[block_of(kind, order[index], me_x)]
        return remote(
            block, block, az_send.at[kind, 1 + index], az_recv.at[kind, slot], {"z": target}
        )

    def a_z_next(kind, index):
        @pl.when(inner)
        def _():
            a_z(kind, index).start()

    def a_z_done(kind):
        @pl.when(last_z == 0)
        def _():
            a_z_own(kind, 1).wait_send()

        @pl.when(first_z == 0)
        def _():
            a_z_own(kind, 0).wait_send()

        @pl.when(inner)
        def _():
            for index in range(1, z_size):
                a_z(kind, index).wait_send()

    def a_z_in(kind, step):
        block = bufs[kind].at[block_of(kind, step, me_x)]
        return remote(block, block, az_send.at[kind, 0], az_recv.at[kind, step], to_z(1))

    def a_x(kind, step):
        return remote(
            source(kind, step),
            bufs[kind].at[block_of(kind, step, me_x)],
            ax_send.at[kind, step],
            ax_recv.at[kind, step],
            to_x,
        )

    def a_x_in(kind, step):
        block = bufs[kind].at[block_of(kind, step, 1 - me_x)]
        return remote(block, block, ax_send.at[kind, step], ax_recv.at[kind, step], to_x)

    def a_c(kind, step, far):
        x_at = 1 - me_x if far else me_x
        block = bufs[kind].at[row_block(step, x_at, me_c)]
        src = source(kind, step) if kind and not far else block
        slot = step + z_size * far
        return remote(src, block, ac_send.at[kind, slot], ac_recv.at[kind, slot], to_c)

    def a_c_in(kind, step, far):
        x_at = 1 - me_x if far else me_x
        block = bufs[kind].at[row_block(step, x_at, 1 - me_c)]
        slot = step + z_size * far
        return remote(block, block, ac_send.at[kind, slot], ac_recv.at[kind, slot], to_c)

    def f_z(kind, step, act):
        target = lax.rem(me_z + step, z_size)

        def piece(index, src, dst):
            return remote(
                ffn_in[kind].at[:, src],
                w3_out.at[kind, here, dst],
                fz_send.at[kind, step, index],
                fz_recv.at[kind, step, index],
                to_z(step),
            )

        act(piece(0, *body_of(target)))

        @pl.when(is_inner(target))
        def _():
            act(piece(1, *tail_of(target)))

    def f_z_wait(kind, step):
        block = row_block(step, me_x, me_c)

        def piece(index, dst):
            part = w3_out.at[kind, block, dst]
            return remote(
                part, part, fz_send.at[kind, step, index], fz_recv.at[kind, step, index], to_z(step)
            )

        piece(0, pl.ds(0, main)).wait_recv()

        @pl.when(inner)
        def _():
            piece(1, pl.ds(main, 128)).wait_recv()

    def f_x(kind, step, x_at, act):
        for case, columns in ((inner, units), (first_z + last_z > 0, main)):

            @pl.when(case)
            def _(columns=columns):
                block = w3_out.at[kind, row_block(step, x_at, me_c), pl.ds(0, columns)]
                act(remote(block, block, fx_send.at[kind, step], fx_recv.at[kind, step], to_x))

    def f_x_start(kind, step):
        f_x(kind, step, me_x, lambda copy: copy.start())

    def f_x_wait(kind, step):
        f_x(kind, step, 1 - me_x, lambda copy: copy.wait_recv())

    def f_x_done(kind, step):
        f_x(kind, step, me_x, lambda copy: copy.wait_send())

    def f_c(kind, step, far):
        block = w3_out.at[kind, row_block(step, 1 - me_x if far else me_x, me_c)]
        slot = step + z_size * far
        return remote(block, block, fc_send.at[kind, slot], fc_recv.at[kind, slot], to_c)

    def f_c_in(kind, step, far):
        block = w3_out.at[kind, row_block(step, 1 - me_x if far else me_x, 1 - me_c)]
        slot = step + z_size * far
        return remote(block, block, fc_send.at[kind, slot], fc_recv.at[kind, slot], to_c)

    def d_source(step):
        return cot_hbm if isinstance(step, int) else dy_out.at[step, mine]

    def d_z_own(right):
        slot = 1 if right else z_size - 1
        return remote(
            cot_hbm, dy_out.at[slot, mine], dz_send.at[right], dz_recv.at[slot], to_z(slot)
        )

    def d_z_start():
        @pl.when(last_z == 0)
        def _():
            d_z_own(1).start()

        @pl.when(first_z == 0)
        def _():
            d_z_own(0).start()

    def d_z(index):
        target, slot = hops[index]
        return remote(
            dy_out.at[order[index], mine],
            dy_out.at[slot, mine],
            dz_send.at[1 + index],
            dz_recv.at[slot],
            {"z": target},
        )

    def d_z_done():
        @pl.when(last_z == 0)
        def _():
            d_z_own(1).wait_send()

        @pl.when(first_z == 0)
        def _():
            d_z_own(0).wait_send()

        @pl.when(inner)
        def _():
            for index in range(1, z_size):
                d_z(index).wait_send()

    def d_z_in(step):
        block = dy_out.at[step, mine]
        return remote(block, block, dz_send.at[0], dz_recv.at[step], to_z(1))

    def d_y(step):
        return remote(
            d_source(step), dy_out.at[step, mine], dy_send.at[step], dy_recv.at[step], to_y
        )

    def d_y_in(step):
        block = dy_out.at[step, theirs]
        return remote(block, block, dy_send.at[step], dy_recv.at[step], to_y)

    for kind in (1, 0, 2):
        a_z_start(kind)
        a_x(kind, 0).start()
    kv_y(0, 0).start()
    tok_y.start()
    for kind in (1, 2):
        a_c(kind, 0, 0).start()

    for at_end, away in ((first_z, 1), (last_z, z_size - 1)):

        @pl.when(at_end > 0)
        def _(away=away):
            for kind in range(3):
                f_z(kind, away, lambda copy: copy.start())

    tok[mine, :] = tok_ref[...]
    seq = 2 * own
    query_at = lax.broadcasted_iota(jnp.int32, (seq, seq), 0)
    key_at = lax.broadcasted_iota(jnp.int32, (seq, seq), 1)
    segment = seg_ref[...].astype(jnp.float32)
    same = jnp.broadcast_to(segment, (8, seq)).T[:, :1] == segment
    allowed = same & (key_at <= query_at) & (query_at - key_at < WINDOW)
    allow_ref[...] = jnp.where(allowed, 1.0, 0.0)
    d_y(0).start()

    def from_x(index):
        step = order[index]
        for kind in (1, 0, 2):
            a_x_in(kind, step).wait_recv()
            if kind:
                a_c(kind, step, 1).start()
            else:
                kv_y(step, 1).start()

    def from_y(index):
        step = order[index]
        for far in range(2):
            kv_y_in(step, far).wait_recv()
            a_c(0, step, far).start()

    for index in range(1, z_size):
        step = order[index]
        for kind in (1, 0, 2):
            a_z_in(kind, step).wait_recv()
            a_z_next(kind, index)
            a_x(kind, step).start()
            if kind:
                a_c(kind, step, 0).start()
            else:
                kv_y(step, 0).start()
        if index == z_size - 2:
            d_z_start()
        if index == z_size - 1:
            for copy in own_f:
                copy.wait()

            @pl.when(inner)
            def _():
                for kind in range(3):
                    own_tail(kind).wait()

            for kind in range(3):
                for away, sent in ((1, first_z), (3, last_z), (2, 0)):

                    @pl.when(sent == 0 if away != 2 else me_z >= 0)
                    def _(kind=kind, away=away):
                        f_z(kind, away, lambda copy: copy.start())

            for kind in range(3):
                f_x_start(kind, 0)
                f_c(kind, 0, 0).start()
        if index >= 2:
            from_x(index - 2)
            from_y(index - 2)
    for index in (z_size - 2, z_size - 1):
        from_x(index)
        from_y(index)

    def hand_on(kind, step):
        f_z_wait(kind, step)
        f_x_start(kind, step)
        f_c(kind, step, 0).start()

    def cross(kind, step):
        f_x_wait(kind, step)
        f_c(kind, step, 1).start()

    def pass_cotangent(step):
        d_z_in(order[step]).wait_recv()

        @pl.when(inner)
        def _():
            d_z(step).start()

        d_y(order[step]).start()

    def pass_if(case, step):
        @pl.when(case)
        def _():
            pass_cotangent(step)

    outer = first_z + last_z > 0
    tok_y_in.wait_recv()
    own_q.wait()
    own_o.wait()
    for kind in (0, 1):
        for step in range(z_size):
            for far in range(2):
                a_c_in(kind, step, far).wait_recv()

    gains = kv_w[:, 2 * head :].astype(jnp.float32).T[:8, :]
    gain_ref[...] = gains

    def norm_rows(index, carry):
        at = pl.ds(pl.multiple_of(index * 32, 32), 32)
        values = tok[at, :].astype(jnp.float32)
        scale = lax.rsqrt(jnp.mean(values * values, axis=-1, keepdims=True) + epsilon)
        n1_ref[at, :] = (values * scale * gain_ref[0:1, :]).astype(jnp.bfloat16)
        return carry

    lax.fori_loop(0, 2 * own // 32, norm_rows, 0)
    hand_on(0, order[1])
    table = (cos_ref[...], sin_ref[...])
    key_ref[...] = spin(dot_nn(n1_ref[...], kv_w[:, :head]), table).astype(jnp.bfloat16)
    val_ref[...] = dot_nn(n1_ref[...], kv_w[:, head : 2 * head]).astype(jnp.bfloat16)
    hand_on(0, order[2])
    head_scale = head ** (-0.5)
    heads = att_ref.shape[1] // head

    half_cols = att_ref.shape[1] // 2
    for index in range(2):
        cols = pl.ds(index * half_cols, half_cols)
        query[:, cols] = dot_nn(n1_ref[...], q_w[:, cols])

    def attend(index):
        cols = pl.ds(index * head, head)
        rotated = (spin(query[:, cols], table) * head_scale).astype(jnp.bfloat16)
        rot_ref[:, cols] = rotated
        probs = head_probs(rotated, key_ref[...], allow_ref[...]).astype(jnp.bfloat16)
        att_ref[:, cols] = dot_nn(probs, val_ref[...]).astype(jnp.bfloat16)

    tasks = [
        lambda: (pass_cotangent(1), pass_if(inner, 2)),
        lambda: hand_on(0, order[3]),
        lambda: (cross(0, 0), hand_on(1, order[1])),
        lambda: cross(1, 0),
        lambda: (cross(2, 0), hand_on(1, order[2])),
    ]
    for index in range(heads):
        attend(index)
        if index < len(tasks):
            tasks[index]()
    for step in range(z_size):
        for far in range(2):
            a_c_in(2, step, far).wait_recv()
    saves = [
        local(kv_w, kv_out),
        local(q_w, wq_out),
        local(o_w, wo_out),
    ]
    span = width // 4

    def project(index, carry):
        cols = pl.ds(pl.multiple_of(index * span, span), span)
        part[:, cols] = matmul_nt(att_ref[...], o_w[cols, :]).astype(jnp.bfloat16)
        return carry

    lax.fori_loop(0, 4, project, 0)
    part_out.start()
    hand_on(1, order[3])
    pass_if(outer, 2)
    pass_if(inner, 3)
    cross(0, order[1])
    hand_on(2, order[1])
    part_out.wait_recv()

    def middle(index, carry):
        at = pl.ds(pl.multiple_of(index * 32, 32), 32)
        there = pl.ds(pl.multiple_of(me_y * own + index * 32, 32), 32)
        values = (
            tok_ref[at, :].astype(jnp.float32)
            + part[there, :].astype(jnp.float32)
            + part_y[at, :].astype(jnp.float32)
        )
        mid_ref[at, :] = values
        scale = lax.rsqrt(jnp.mean(values * values, axis=-1, keepdims=True) + epsilon)
        n2_ref[there, :] = (values * scale * gain_ref[1:2, :]).astype(jnp.bfloat16)
        return carry

    lax.fori_loop(0, own // 32, middle, 0)
    n2_y.start()
    hand_on(2, order[2])
    cross(0, order[2])
    cross(0, order[3])
    hand_on(2, order[3])
    pass_if(outer, 3)
    for kind in (1, 2):
        for index in (1, 2, 3):
            cross(kind, order[index])
    for kind in range(3):
        for step in range(z_size):
            for far in range(2):
                f_c_in(kind, step, far).wait_recv()
        saves.append(local(w3_out.at[kind], w3_save.at[kind]))
    for step in range(z_size):
        d_y_in(step).wait_recv()
    own_d.wait()
    saves.append(local(dy_out, dy_save))
    n2_y_in.wait_recv()

    for kind in range(3):
        a_z_done(kind)
    d_z_done()
    tok_y.wait_send()
    part_out.wait_send()
    n2_y.wait_send()
    for copy in saves:
        copy.wait()
    for step in range(z_size):
        d_y(step).wait_send()
        for far in range(2):
            kv_y(step, far).wait_send()
        for kind in range(3):
            if step:
                f_z(kind, step, lambda copy: copy.wait_send())
            a_x(kind, step).wait_send()
            f_x_done(kind, step)
            for far in range(2):
                a_c(kind, step, far).wait_send()
                f_c(kind, step, far).wait_send()


def pre_call(
    tokens, w_kv, gain_one, gain_two, table, segments, cotangent, w_query, w_out, ffn
):
    z_size = lax.axis_size("z")
    own, width = tokens.shape
    seq = 2 * own
    rows, cols = w_query.shape
    head = table[0].shape[1] * 2
    units = ragged_split(ffn[0].shape[1], z_size)[1]
    low = lambda *dims: jax.ShapeDtypeStruct(dims, jnp.bfloat16)
    full = lambda *dims: jax.ShapeDtypeStruct(dims, jnp.float32)
    dma = lambda *lead: pltpu.SemaphoreType.DMA(lead)
    vmem = pl.BlockSpec(memory_space=pltpu.VMEM)
    hbm = pl.BlockSpec(memory_space=pl.ANY)
    wide = lambda *lead: pltpu.VMEM((*lead, width), jnp.bfloat16)
    return pl.pallas_call(
        functools.partial(pre_kernel, z_size),
        out_shape=(
            low(seq, width),
            low(seq, cols),
            low(seq, head),
            low(seq, head),
            low(seq, cols),
            full(own, width),
            low(seq, width),
            full(8, width),
            full(seq, seq),
            low(width, 2 * head + 128),
            low(width, cols),
            low(width, cols),
            low(3, width, units),
            low(z_size, seq, width),
        ),
        in_specs=[vmem] * 7 + [hbm] * 6,
        out_specs=(vmem,) * 9 + (hbm,) * 5,
        scratch_shapes=[
            pltpu.VMEM((3, width, units), jnp.bfloat16),
            wide(z_size, seq),
            pltpu.VMEM((width, 2 * head + 128), jnp.bfloat16),
            pltpu.VMEM((width, cols), jnp.bfloat16),
            pltpu.VMEM((width, cols), jnp.bfloat16),
            wide(seq),
            wide(seq),
            wide(own),
            pltpu.VMEM((seq, cols), jnp.float32),
            pltpu.VMEM((128, 128), jnp.float32),
            dma(4),
            dma(4),
            dma(2 * z_size),
            dma(2 * z_size),
            dma(3, z_size + 1),
            dma(3, z_size),
            dma(3, z_size),
            dma(3, z_size),
            dma(3, 2 * z_size),
            dma(3, 2 * z_size),
            dma(3, z_size, 2),
            dma(3, z_size, 2),
            dma(3, z_size),
            dma(3, z_size),
            dma(3, 2 * z_size),
            dma(3, 2 * z_size),
            dma(z_size + 1),
            dma(z_size),
            dma(z_size),
            dma(z_size),
            dma(24),
        ],
        compiler_params=pltpu.CompilerParams(
            collective_id=1, has_side_effects=True, vmem_limit_bytes=VMEM_BYTES
        ),
        cost_estimate=pl.CostEstimate(
            flops=8 * seq * width * cols,
            bytes_accessed=8 * width * (cols + units),
            transcendentals=seq * seq * cols // head,
        ),
    )(tokens, w_kv, gain_one, gain_two, *table, segments, cotangent, w_query, w_out, *ffn)


def post_kernel(
    z_size,
    main,
    tok_ref,
    gain_ref,
    gain_part_ref,
    n1_ref,
    rot_ref,
    key_ref,
    val_ref,
    att_ref,
    cos_ref,
    sin_ref,
    allow_ref,
    kv_hbm,
    wq_hbm,
    wo_hbm,
    mix_hbm,
    gmf_hbm,
    gmb_hbm,
    mid_hbm,
    sums_hbm,
    mixed_ref,
    tgrad_ref,
    gsum_ref,
    kvg_ref,
    qg_ref,
    og_ref,
    ffn_out,
    kv_w,
    q_w,
    o_w,
    o_part,
    gm,
    gm_f,
    gq,
    gkv,
    kv_sum,
    back_y,
    mix_y,
    mix_z,
    mix_s,
    o_c,
    o_x,
    o_z,
    q_c,
    q_x,
    q_z,
    kv_y,
    kv_c,
    kv_x,
    kv_z,
    gain_own,
    gain_in,
    ffn_in,
    ffn_own,
    ffn_go,
    load_sem,
    own_sem,
    go_sem,
    fx_send,
    fx_recv,
    fz_send,
    fz_recv,
    y_send,
    y_recv,
    my_send,
    my_recv,
    mz_send,
    mz_recv,
    wc_send,
    wc_recv,
    wx_send,
    wx_recv,
    wz_send,
    wz_recv,
    kc_send,
    kc_recv,
    kz_send,
    kz_recv,
    g_send,
    g_recv,
):
    me_z, me_x = lax.axis_index("z"), lax.axis_index("x")
    me_c, me_y = lax.axis_index("c"), lax.axis_index("mp")
    own, width = tok_ref.shape
    seq = 2 * own
    head = key_ref.shape[1]
    cols_here = att_ref.shape[1]
    heads = cols_here // head
    rows = qg_ref.shape[0]
    span = width // z_size
    mine = pl.ds(pl.multiple_of(me_y * own, own), own)
    theirs = pl.ds(pl.multiple_of((1 - me_y) * own, own), own)
    to_y, to_x, to_c = {"mp": 1 - me_y}, {"x": 1 - me_x}, {"c": 1 - me_c}
    head_scale = head ** (-0.5)

    def behind(step):
        return lax.rem(me_z - step + z_size, z_size)

    def to_z(step):
        return {"z": lax.rem(me_z + step, z_size)}

    def row_block(step, x_at, c_at):
        start = ((behind(step) * 2 + x_at) * 2 + c_at) * rows
        return pl.ds(pl.multiple_of(start, rows), rows)

    loads = [
        pltpu.make_async_copy(wo_hbm, o_w, load_sem.at[0]),
        pltpu.make_async_copy(wq_hbm, q_w, load_sem.at[1]),
        pltpu.make_async_copy(
            kv_hbm.at[:, :, :, :, :, pl.ds(0, 2 * head)], kv_w, load_sem.at[2]
        ),
    ]
    for step in range(z_size):
        loads.append(
            pltpu.make_async_copy(mix_hbm.at[step, me_y], mix_s.at[step], load_sem.at[3 + step])
        )
    loads.append(pltpu.make_async_copy(gmf_hbm, gm_f, load_sem.at[3 + z_size]))
    loads.append(pltpu.make_async_copy(gmb_hbm, gm.at[mine], load_sem.at[4 + z_size]))
    mid_load = pltpu.make_async_copy(mid_hbm, gm_f, load_sem.at[5 + z_size])
    for load in loads:
        load.start()

    def go(kind, step, far):
        return pltpu.make_async_copy(sums_hbm.at[kind, step, far], ffn_go.at[kind], go_sem.at[kind])

    go_first = [go(kind, 1, 0) for kind in range(3)]
    for copy in go_first:
        copy.start()

    barrier = pltpu.get_barrier_semaphore()
    peers = [to_y, to_x, to_c] + [to_z(step) for step in range(1, z_size)]
    for where in peers:
        pl.semaphore_signal(barrier, inc=1, device_id=where, device_id_type=MESH_ID)
    pl.semaphore_wait(barrier, len(peers))

    tasks = [(step, kind) for step in (2, 3) for kind in range(3)]

    def f_x(index):
        step, kind = tasks[index]
        return remote(
            sums_hbm.at[kind, step, 1],
            ffn_in.at[index],
            fx_send.at[index],
            fx_recv.at[index],
            to_x,
        )

    def f_own(index):
        step, kind = tasks[index]
        return pltpu.make_async_copy(
            sums_hbm.at[kind, step, 0], ffn_own, own_sem.at[0]
        )

    def f_z(step, kind, source_z, act):
        for case, columns in (
            ((source_z > 0) & (source_z < z_size - 1), ffn_out.shape[3]),
            ((source_z == 0) | (source_z == z_size - 1), main),
        ):

            @pl.when(case)
            def _(columns=columns):
                cols = pl.ds(0, columns)
                if step == 1:
                    src = ffn_go.at[kind, :, cols]
                else:
                    src = ffn_in.at[tasks.index((step, kind)), :, cols]
                act(
                    remote(
                        src,
                        ffn_out.at[kind, step, :, cols],
                        fz_send.at[kind, step],
                        fz_recv.at[kind, step],
                        to_z(step),
                    )
                )

    def tick(index):
        step, kind = tasks[index]
        f_x(index).wait_recv()
        f_own(index).wait()
        block = ffn_in.at[index]
        add_rows(block, [ffn_own], block, rows)
        if index + 1 < len(tasks):
            f_own(index + 1).start()
        f_z(step, kind, me_z, lambda copy: copy.start())

    def f_x_own(kind):
        return remote(
            ffn_go.at[kind],
            ffn_out.at[kind, 0],
            fx_send.at[len(tasks) + kind],
            fx_recv.at[len(tasks) + kind],
            to_x,
        )

    f_own(0).start()
    for index in range(len(tasks)):
        f_x(index).start()
    for kind in range(3):
        go_first[kind].wait()
        f_z(1, kind, me_z, lambda copy: copy.start())

    gm_y = remote(gmb_hbm, gm.at[mine], y_send.at[0], y_recv.at[0], to_y)
    gm_y_in = remote(gm.at[theirs], gm.at[theirs], y_send.at[0], y_recv.at[0], to_y)
    gm_y.start()

    first_z, last_z = (z_size - 1 - me_z) // (z_size - 1), me_z // (z_size - 1)
    inner = first_z + last_z == 0
    order = (
        0,
        1 + (me_z + 1) // 2,
        2 + (2 * me_z - 3) * (1 - first_z - last_z),
        3 - 2 * (me_z // 2),
    )
    right = (None, 1 - me_z // 2, (3 - me_z) * (2 - me_z) // 6 + me_z // 2 * (1 - last_z), 1 - me_z // 2)

    def hop_slot(index):
        step, way = order[index], right[index]
        return way * lax.rem(step + 1, z_size) + (1 - way) * (step - 1 + 4 * ((3 - step) // 2))

    def hop_target(index):
        return {"z": me_z + 2 * right[index] - 1}

    def mix_over_y(step):
        return remote(
            mix_hbm.at[step, 1 - me_y], mix_y.at[step], my_send.at[step], my_recv.at[step], to_y
        )

    def mix_over_z(index):
        slot = hop_slot(index)
        return remote(
            mix_s.at[order[index]],
            mix_z.at[slot],
            mz_send.at[index],
            mz_recv.at[slot],
            hop_target(index),
        )

    def mix_z_in(slot):
        return remote(mix_z.at[slot], mix_z.at[slot], mz_send.at[1], mz_recv.at[slot], to_z(1))

    def mix_add(step, others, last):
        def add_tile(tile, carry):
            at = pl.ds(pl.multiple_of(tile * TILE, TILE), TILE)
            total = mix_s[step, at, :].astype(jnp.float32)
            for other in others:
                total = total + other[at, :].astype(jnp.float32)
            if last:
                mixed_ref[:, at] = (gm_f[:, at] + total.T).astype(jnp.bfloat16)
            else:
                mix_s[step, at, :] = total.astype(jnp.bfloat16)
            return carry

        lax.fori_loop(0, width // TILE, add_tile, 0)

    def mix_step(index):
        step = order[index]
        mix_over_y(step).wait_recv()
        from_y = mix_y.at[step]
        if index:

            @pl.when(inner)
            def _():
                mix_z_in(step).wait_recv()
                mix_add(step, [from_y, mix_z.at[step]], False)

            @pl.when(first_z + last_z > 0)
            def _():
                mix_add(step, [from_y], False)

            mix_over_z(index).start()
        else:
            mid_load.wait()

            @pl.when(first_z == 0)
            def _():
                mix_z_in(0).wait_recv()

            @pl.when(last_z == 0)
            def _():
                mix_z_in(z_size).wait_recv()

            @pl.when(inner)
            def _():
                mix_add(0, [from_y, mix_z.at[0], mix_z.at[z_size]], True)

            @pl.when(first_z > 0)
            def _():
                mix_add(0, [from_y, mix_z.at[z_size]], True)

            @pl.when(last_z > 0)
            def _():
                mix_add(0, [from_y, mix_z.at[0]], True)

    for index in (1, 2, 3, 0):
        mix_over_y(order[index]).start()

    kinds = ((o_part, o_c, o_x, o_z, og_ref), (o_w, q_c, q_x, q_z, qg_ref))

    def w_c(kind, step, far):
        x_at = 1 - me_x if far else me_x
        return remote(
            kinds[kind][0].at[row_block(step, x_at, 1 - me_c)],
            kinds[kind][1].at[step, far],
            wc_send.at[kind, step, far],
            wc_recv.at[kind, step, far],
            to_c,
        )

    def w_x(kind, step):
        return remote(
            kinds[kind][0].at[row_block(step, 1 - me_x, me_c)],
            kinds[kind][2].at[step],
            wx_send.at[kind, step],
            wx_recv.at[kind, step],
            to_x,
        )

    def w_z(kind, index):
        step, slot = order[index], hop_slot(index)
        return remote(
            kinds[kind][0].at[row_block(step, me_x, me_c)],
            kinds[kind][3].at[slot],
            wz_send.at[kind, index],
            wz_recv.at[kind, slot],
            hop_target(index),
        )

    def w_z_in(kind, slot):
        block = kinds[kind][3].at[slot]
        return remote(block, block, wz_send.at[kind, 1], wz_recv.at[kind, slot], to_z(1))

    def w_x_stage(kind, index):
        step = order[index]
        w_c(kind, step, 1).wait_recv()
        block = kinds[kind][0].at[row_block(step, 1 - me_x, me_c)]
        add_rows(block, [kinds[kind][1].at[step, 1]], block, rows)
        w_x(kind, step).start()

    def w_z_stage(kind, index):
        part, from_c, from_x, from_z, result = kinds[kind]
        step = order[index]
        w_c(kind, step, 0).wait_recv()
        w_x(kind, step).wait_recv()
        block = part.at[row_block(step, me_x, me_c)]
        others = [from_c.at[step, 0], from_x.at[step]]
        if index:

            @pl.when(inner)
            def _():
                w_z_in(kind, step).wait_recv()
                add_rows(block, [*others, from_z.at[step]], block, rows)

            @pl.when(first_z + last_z > 0)
            def _():
                add_rows(block, others, block, rows)

            w_z(kind, index).start()
        else:

            @pl.when(first_z == 0)
            def _():
                w_z_in(kind, 0).wait_recv()

            @pl.when(last_z == 0)
            def _():
                w_z_in(kind, z_size).wait_recv()

            @pl.when(inner)
            def _():
                add_rows(block, [*others, from_z.at[0], from_z.at[z_size]], result, rows)

            @pl.when(first_z > 0)
            def _():
                add_rows(block, [*others, from_z.at[z_size]], result, rows)

            @pl.when(last_z > 0)
            def _():
                add_rows(block, [*others, from_z.at[0]], result, rows)

    def w_product(kind, index, left, values):
        step = order[index]
        at = pl.ds(pl.multiple_of(behind(step) * span, 128), span)
        turned = left[:, at].T

        def tile_body(tile, carry):
            cols = pl.ds(pl.multiple_of(tile * TILE, TILE), TILE)
            kinds[kind][0][at, cols] = dot_nn(turned, values[:, cols]).astype(jnp.bfloat16)
            return carry

        lax.fori_loop(0, cols_here // TILE, tile_body, 0)
        for far in (1, 0):
            w_c(kind, step, far).start()

    tick(0)
    tick(1)
    loads[-1].wait()
    gm_y_in.wait_recv()
    w_product(0, 1, gm, att_ref)
    w_product(0, 2, gm, att_ref)
    w_x_stage(0, 1)
    w_product(0, 3, gm, att_ref)
    w_x_stage(0, 2)
    tick(2)
    w_product(0, 0, gm, att_ref)
    w_x_stage(0, 3)
    for load in loads[:-1]:
        load.wait()

    kv_sum[...] = jnp.zeros(kv_sum.shape, jnp.float32)
    table = (cos_ref[...], sin_ref[...])

    for index in range(2):
        cols = pl.ds(index * (cols_here // 2), cols_here // 2)
        gq[:, cols] = dot_nn(gm[...], o_w[:, cols]).astype(jnp.bfloat16)

    def attend_back(index):
        cols = pl.ds(index * head, head)
        grad_vals = gq[:, cols]
        rotated = rot_ref[:, cols]
        probs = head_probs(rotated, key_ref[...], allow_ref[...])
        grad_probs = matmul_nt(grad_vals, val_ref[...])
        delta = jnp.sum(probs * grad_probs, axis=-1, keepdims=True)
        grad_scores = (probs * (grad_probs - delta)).astype(jnp.bfloat16)
        grad_rot = dot_nn(grad_scores, key_ref[...])
        gq[:, cols] = (spin_back(grad_rot, table) * head_scale).astype(jnp.bfloat16)
        kv_sum[0] += matmul_tn(grad_scores, rotated)
        kv_sum[1] += matmul_tn(probs.astype(jnp.bfloat16), grad_vals)

    for index in range(heads):
        attend_back(index)
        if index == 0:
            w_x_stage(0, 0)
        if 3 + index < len(tasks):
            tick(3 + index)
        if index == heads - 1:
            mix_step(1)
    gkv[:, :head] = spin_back(kv_sum[0], table).astype(jnp.bfloat16)
    gkv[:, head:] = kv_sum[1].astype(jnp.bfloat16)

    w_product(1, 1, n1_ref, gq)
    w_product(1, 2, n1_ref, gq)
    w_x_stage(1, 1)
    w_z_stage(0, 1)
    w_product(1, 3, n1_ref, gq)
    w_x_stage(1, 2)
    w_product(1, 0, n1_ref, gq)
    w_x_stage(1, 3)
    w_x_stage(1, 0)
    for kind in range(3):
        f_z(1, kind, me_z, lambda copy: copy.wait_send())
        go(kind, 0, 1).start()
    for kind in range(3):
        go(kind, 0, 1).wait()
        f_x_own(kind).start()

    gm_y.wait_send()
    back = gm
    def input_tile(index, carry):
        at = pl.ds(pl.multiple_of(index * span, 128), span)
        back[:, at] = (
            matmul_nt(gq[...], q_w[at, :]) + matmul_nt(gkv[...], kv_w[index].reshape(span, 2 * head))
        ).astype(jnp.bfloat16)
        return carry

    lax.fori_loop(0, z_size, input_tile, 0)
    back_out = remote(back.at[theirs], back_y, y_send.at[1], y_recv.at[1], to_y)
    back_out.start()

    kv_part = kv_w

    def kv_tile(index, carry):
        at = pl.ds(pl.multiple_of(index * span, 128), span)
        product = dot_nn(n1_ref[:, at].T, gkv[...]).astype(jnp.bfloat16)
        kv_part[index] = product.reshape(kv_part.shape[1:])
        return carry

    lax.fori_loop(0, z_size, kv_tile, 0)
    kv_over_y = remote(kv_part.at[:, :, :, 1 - me_y], kv_y, y_send.at[2], y_recv.at[2], to_y)
    kv_over_y.start()
    mix_step(2)
    w_z_stage(0, 2)
    mix_step(3)
    w_z_stage(0, 3)

    back_out.wait_recv()

    def input_rows(index, total):
        at = pl.ds(pl.multiple_of(index * 32, 32), 32)
        there = pl.ds(pl.multiple_of(me_y * own + index * 32, 32), 32)
        upstream = back[there, :].astype(jnp.float32) + back_y[at, :].astype(jnp.float32)
        grad, gain_part = norm_back(
            tok_ref[at, :].astype(jnp.float32), gain_ref[0:1, :], upstream
        )
        tgrad_ref[at, :] = (gm_f[at, :] + grad).astype(jnp.bfloat16)
        return total + gain_part

    attn_gain_part = lax.fori_loop(
        0, own // 32, input_rows, jnp.zeros((1, width), jnp.float32)
    )
    for index in range(4):
        at = slice(index * span, (index + 1) * span)
        gain_own[0, index : index + 1, :] = attn_gain_part[:, at]
        gain_own[0, 4 + index : 5 + index, :] = gain_part_ref[4 + index : 5 + index, :]

    def gain_send(stage, where):
        return remote(
            gain_own.at[stage], gain_in.at[stage], g_send.at[stage], g_recv.at[stage], where
        )

    gain_hops = [gain_send(0, to_y), gain_send(1, to_c), gain_send(2, to_x)]
    gain_last = [
        remote(
            gain_own.at[3], gain_in.at[2 + step], g_send.at[2 + step], g_recv.at[2 + step], to_z(step)
        )
        for step in range(1, z_size)
    ]

    def gain_fold(stage):
        gain_hops[stage].wait_recv()
        gain_own[stage + 1] = gain_own[stage] + gain_in[stage]

    gain_hops[0].start()
    mid_load.start()
    w_z_stage(1, 1)
    w_z_stage(0, 0)
    w_z_stage(1, 2)
    gain_fold(0)
    gain_hops[1].start()
    mix_step(0)
    w_z_stage(1, 3)
    gain_fold(1)
    gain_hops[2].start()
    kv_over_y.wait_recv()

    def kv_add_y(index, carry):
        for x_at in range(2):
            for c_at in range(2):
                block = kv_part.at[index, x_at, c_at, me_y]
                block[...] = (
                    block[...].astype(jnp.float32) + kv_y[index, x_at, c_at].astype(jnp.float32)
                ).astype(jnp.bfloat16)
        return carry

    lax.fori_loop(0, z_size, kv_add_y, 0)
    kv_over_c = remote(
        kv_part.at[:, :, 1 - me_c, me_y], kv_c, kc_send.at[0], kc_recv.at[0], to_c
    )
    kv_over_c.start()
    gain_fold(2)
    for copy in gain_last:
        copy.start()
    kv_over_c.wait_recv()

    def kv_add_c(index, carry):
        for x_at in range(2):
            block = kv_part.at[index, x_at, me_c, me_y]
            block[...] = (
                block[...].astype(jnp.float32) + kv_c[index, x_at].astype(jnp.float32)
            ).astype(jnp.bfloat16)
        return carry

    lax.fori_loop(0, z_size, kv_add_c, 0)
    kv_over_x = remote(
        kv_part.at[:, 1 - me_x, me_c, me_y], kv_x, kc_send.at[1], kc_recv.at[1], to_x
    )
    kv_over_x.start()
    w_z_stage(1, 0)
    kv_over_x.wait_recv()

    def kv_add_x(index, carry):
        block = kv_part.at[index, me_x, me_c, me_y]
        block[...] = (
            block[...].astype(jnp.float32) + kv_x[index].astype(jnp.float32)
        ).astype(jnp.bfloat16)
        return carry

    lax.fori_loop(0, z_size, kv_add_x, 0)
    kv_over_z = [
        remote(
            kv_part.at[lax.rem(me_z + step, z_size), me_x, me_c, me_y],
            kv_z.at[step - 1],
            kz_send.at[step],
            kz_recv.at[step],
            to_z(step),
        )
        for step in range(1, z_size)
    ]
    for copy in kv_over_z:
        copy.start()
    for copy in gain_last:
        copy.wait_recv()
    gsum_ref[...] = gain_own[3] + gain_in[3] + gain_in[4] + gain_in[5]
    for copy in kv_over_z:
        copy.wait_recv()
    kvg_ref[...] = (
        kv_part[me_z, me_x, me_c, me_y].astype(jnp.float32)
        + kv_z[0].astype(jnp.float32)
        + kv_z[1].astype(jnp.float32)
        + kv_z[2].astype(jnp.float32)
    )

    back_out.wait_send()
    kv_over_y.wait_send()
    kv_over_c.wait_send()
    kv_over_x.wait_send()
    for kind in range(3):
        f_x_own(kind).wait()
    for index in range(len(tasks)):
        f_x(index).wait_send()
    for step in range(1, z_size):
        for kind in range(3):
            if step > 1:
                f_z(step, kind, me_z, lambda copy: copy.wait_send())
            f_z(step, kind, behind(step), lambda copy: copy.wait_recv())
    for copy in gain_hops + gain_last + kv_over_z:
        copy.wait_send()
    for step in range(z_size):
        mix_over_y(step).wait_send()
        if step:
            mix_over_z(step).wait_send()
        for kind in range(2):
            w_c(kind, step, 0).wait_send()
            w_c(kind, step, 1).wait_send()
            w_x(kind, step).wait_send()
            if step:
                w_z(kind, step).wait_send()


def post_call(
    tokens,
    gains,
    gain_part,
    normed_one,
    rotated,
    keys,
    values,
    attn_vals,
    table,
    allowed,
    kv_weight,
    query_weight,
    out_weight,
    mix_parts,
    grad_mid,
    grad_mid_low,
    mid,
    ffn_sums,
    main,
):
    z_size = lax.axis_size("z")
    own, width = tokens.shape
    seq = 2 * own
    head = keys.shape[1]
    cols = attn_vals.shape[1]
    rows = width // (4 * z_size)
    units = ffn_sums.shape[4]
    low = lambda *dims: pltpu.VMEM(dims, jnp.bfloat16)
    full = lambda *dims: pltpu.VMEM(dims, jnp.float32)
    out_full = lambda *dims: jax.ShapeDtypeStruct(dims, jnp.float32)
    out_low = lambda *dims: jax.ShapeDtypeStruct(dims, jnp.bfloat16)
    dma = lambda *lead: pltpu.SemaphoreType.DMA(lead)
    vmem = pl.BlockSpec(memory_space=pltpu.VMEM)
    hbm = pl.BlockSpec(memory_space=pl.ANY)
    z = z_size
    return pl.pallas_call(
        functools.partial(post_kernel, z_size, main),
        out_shape=(
            out_low(own, width),
            out_low(own, width),
            out_full(8, width // z),
            out_full(rows // 2, 2 * head),
            out_full(rows, cols),
            out_full(rows, cols),
            out_low(3, z, rows, units),
        ),
        in_specs=[vmem] * 11 + [hbm] * 8,
        out_specs=(vmem,) * 6 + (hbm,),
        scratch_shapes=[
            low(z, 2, 2, 2, rows // 2, 2 * head),
            low(width, cols),
            low(width, cols),
            low(width, cols),
            low(seq, width),
            full(own, width),
            low(seq, cols),
            low(seq, 2 * head),
            full(2, seq, head),
            low(own, width),
            low(z, width, own),
            low(z + 1, width, own),
            low(z, width, own),
            low(z, 2, rows, cols),
            low(z, rows, cols),
            low(z + 1, rows, cols),
            low(z, 2, rows, cols),
            low(z, rows, cols),
            low(z + 1, rows, cols),
            low(z, 2, 2, rows // 2, 2 * head),
            low(z, 2, rows // 2, 2 * head),
            low(z, rows // 2, 2 * head),
            low(z - 1, rows // 2, 2 * head),
            full(4, 8, width // z),
            full(6, 8, width // z),
            low(6, rows, units),
            low(rows, units),
            low(3, rows, units),
            dma(6 + z),
            dma(1),
            dma(3),
            dma(9),
            dma(9),
            dma(3, z),
            dma(3, z),
            dma(3),
            dma(3),
            dma(z),
            dma(z),
            dma(z),
            dma(z + 1),
            dma(2, z, 2),
            dma(2, z, 2),
            dma(2, z),
            dma(2, z),
            dma(2, z),
            dma(2, z + 1),
            dma(2),
            dma(2),
            dma(z),
            dma(z),
            dma(6),
            dma(6),
        ],
        compiler_params=pltpu.CompilerParams(
            collective_id=2, has_side_effects=True, vmem_limit_bytes=VMEM_BYTES
        ),
        cost_estimate=pl.CostEstimate(
            flops=14 * seq * width * cols,
            bytes_accessed=10 * width * cols,
            transcendentals=seq * seq * cols // head,
        ),
    )(
        tokens,
        gains,
        gain_part,
        normed_one,
        rotated,
        keys,
        values,
        attn_vals,
        *table,
        allowed,
        kv_weight.reshape(z, 2, 2, 2, rows // 2, kv_weight.shape[1]),
        query_weight,
        out_weight,
        mix_parts,
        grad_mid,
        grad_mid_low,
        mid,
        ffn_sums,
    )


def layout_kernel(
    z_size,
    main,
    sum_ref,
    ffn_ref,
    q_ref,
    o_ref,
    kv_ref,
    mixed_in,
    tgrad_in,
    wg_ref,
    wu_ref,
    wd_ref,
    qg_ref,
    og_ref,
    kvg_ref,
    mixed_ref,
    tgrad_ref,
):
    me_z = lax.axis_index("z")
    for kind, out in enumerate((wg_ref, wu_ref, wd_ref)):
        for step in range(z_size):
            at = lax.rem(me_z - step + z_size, z_size)
            values = ffn_ref[kind, step].astype(jnp.float32)
            if step == 0:
                values = values + sum_ref[kind, 0, 0].astype(jnp.float32)
            body = pl.ds(pl.multiple_of(at * main, 128), main)
            out[:, body] = values[:, :main]

            @pl.when((at > 0) & (at < z_size - 1))
            def _(out=out, at=at, values=values):
                tail = z_size * main + lax.rem(at + 1, 2) * 128
                out[:, pl.ds(pl.multiple_of(tail, 128), 128)] = values[:, main:]
    qg_ref[...] = q_ref[...]
    og_ref[...] = o_ref[...]
    kvg_ref[...] = kv_ref[...]
    mixed_ref[...] = mixed_in[...]
    tgrad_ref[...] = tgrad_in[...]


def layout_call(ffn_sums, ffn_grads, query_grad, out_grad, kv_grad, mixed, tokens_grad, ffn_cols):
    z_size = lax.axis_size("z")
    main, units = ragged_split(ffn_cols, z_size)
    rows, cols = query_grad.shape
    parts = rows // 32
    kv_rows = kv_grad.shape[0] // parts
    full = lambda *dims: jax.ShapeDtypeStruct(dims, jnp.float32)
    row = lambda height, width: pl.BlockSpec((height, width), lambda index: (index, 0))
    own, width = mixed.shape
    share = pl.BlockSpec((own, width // parts), lambda index: (0, index))
    specs = [row(32, cols), row(32, cols), row(kv_rows, kv_grad.shape[1]), share, share]
    return pl.pallas_call(
        functools.partial(layout_kernel, z_size, main),
        grid=(parts,),
        out_shape=(
            *[full(rows, ffn_cols)] * 3,
            full(rows, cols),
            full(rows, cols),
            full(*kv_grad.shape),
            jax.ShapeDtypeStruct(mixed.shape, jnp.bfloat16),
            jax.ShapeDtypeStruct(mixed.shape, jnp.bfloat16),
        ),
        in_specs=[
            pl.BlockSpec((3, 1, 1, 32, units), lambda index: (0, 0, 0, index, 0)),
            pl.BlockSpec((3, z_size, 32, units), lambda index: (0, 0, index, 0)),
            *specs,
        ],
        out_specs=(*[row(32, ffn_cols)] * 3, *specs),
        compiler_params=pltpu.CompilerParams(vmem_limit_bytes=VMEM_BYTES),
    )(ffn_sums, ffn_grads, query_grad, out_grad, kv_grad, mixed, tokens_grad)


FF_SPLIT = 4


def ffn_pass(normed, grad_out, gate_weight, up_weight, down_weight):
    gate = jnp.dot(normed, gate_weight, preferred_element_type=jnp.float32)
    up_proj = jnp.dot(normed, up_weight, preferred_element_type=jnp.float32)
    grad_hidden = jnp.dot(grad_out, down_weight, preferred_element_type=jnp.float32)
    product, pull = jax.vjp(gelu_product, gate, up_proj)
    hidden = product.astype(jnp.bfloat16)
    grad_gate_f, grad_up_f = pull(grad_hidden)
    grad_gate = grad_gate_f.astype(jnp.bfloat16)
    grad_up = grad_up_f.astype(jnp.bfloat16)
    mixed_part = matmul_nt(hidden, down_weight).astype(jnp.bfloat16)
    normed_part = (matmul_nt(grad_gate, gate_weight) + matmul_nt(grad_up, up_weight)).astype(
        jnp.bfloat16
    )
    weight_parts = [
        matmul_tn(normed, grad_gate).astype(jnp.bfloat16),
        matmul_tn(normed, grad_up).astype(jnp.bfloat16),
        matmul_tn(grad_out, hidden).astype(jnp.bfloat16),
    ]
    return mixed_part, normed_part, weight_parts


def shards_general(
    tokens,
    segments,
    positions,
    cotangent,
    attn_gain,
    ffn_gain,
    w_kv,
    w_query,
    w_out,
    w_gate,
    w_up,
    w_down,
):
    everywhere = ("z", "xc", "mp")
    dp = ("z", "xc")
    z_size = lax.axis_size("z")
    xc_size = lax.axis_size("xc")
    gains = lax.all_gather(
        jnp.stack([attn_gain, ffn_gain], axis=1), everywhere, axis=0, tiled=True
    ).astype(jnp.float32)
    gain_one, gain_two = gains[:, 0], gains[:, 1]
    kv_weight = lax.all_gather(w_kv, everywhere, axis=0, tiled=True)
    head_dim = kv_weight.shape[1] // 2
    width = tokens.shape[1]
    seq_len = segments.shape[0]
    heads_here = w_query.shape[1] // head_dim
    scale = head_dim ** (-0.5)
    cosine, sine = rotary_angles(positions, head_dim)
    inputs_f = tokens.astype(jnp.float32)
    tokens_all = lax.all_gather(tokens, "mp", axis=0, tiled=True)
    normed_one = norm_gain(tokens_all.astype(jnp.float32), gain_one).astype(jnp.bfloat16)
    query_weight = lax.all_gather(w_query, dp, axis=0, tiled=True)
    out_weight = lax.all_gather(w_out, dp, axis=0, tiled=True)

    rows = w_gate.shape[0]
    unit = w_gate.shape[1] // z_size

    def spread(weight):
        pieces = weight.reshape(rows, z_size, unit).transpose(1, 0, 2)
        pieces = lax.all_to_all(pieces, "z", split_axis=0, concat_axis=0, tiled=True)
        return lax.all_gather(pieces, "xc", axis=1, tiled=False).reshape(width, unit)

    gate_weight, up_weight, down_weight = spread(w_gate), spread(w_up), spread(w_down)
    grad_all = lax.all_gather(cotangent, ("z", "mp"), axis=0, tiled=True)

    query = jnp.dot(normed_one, query_weight, preferred_element_type=jnp.float32).reshape(
        seq_len, heads_here, head_dim
    )
    rotated = (rotate(query, cosine[:, None], sine[:, None]) * scale).astype(jnp.bfloat16)
    keyval = jnp.dot(normed_one, kv_weight, preferred_element_type=jnp.float32)
    keys = rotate(keyval[:, :head_dim], cosine, sine).astype(jnp.bfloat16)
    values = keyval[:, head_dim:].astype(jnp.bfloat16)
    allowed = block_allowed(segments, 0, seq_len)
    scores = jnp.einsum("thd,sd->hts", rotated, keys, preferred_element_type=jnp.float32)
    scores = jnp.where(allowed[None], scores, masked_score)
    row_max = jnp.max(scores, axis=-1, keepdims=True)
    weights = jnp.exp(scores - row_max)
    probs = weights / jnp.sum(weights, axis=-1, keepdims=True)
    probs_low = probs.astype(jnp.bfloat16)
    attn_vals = (
        jnp.einsum("hts,sd->thd", probs_low, values, preferred_element_type=jnp.float32)
        .reshape(seq_len, heads_here * head_dim)
        .astype(jnp.bfloat16)
    )
    mid = inputs_f + lax.psum_scatter(
        matmul_nt(attn_vals, out_weight).astype(jnp.bfloat16),
        "mp",
        scatter_dimension=0,
        tiled=True,
    ).astype(jnp.float32)
    normed_two = norm_gain(mid, gain_two).astype(jnp.bfloat16)
    normed_all = lax.all_gather(normed_two, ("z", "mp"), axis=0, tiled=True)

    mixed_part, normed_part, weight_parts = ffn_pass(
        normed_all, grad_all, gate_weight, up_weight, down_weight
    )
    grad_normed_two = lax.psum_scatter(
        normed_part, ("z", "mp"), scatter_dimension=0, tiled=True
    ).astype(jnp.float32)
    mixed = (
        mid
        + lax.psum_scatter(mixed_part, ("z", "mp"), scatter_dimension=0, tiled=True).astype(
            jnp.float32
        )
    ).astype(jnp.bfloat16)

    def collect(part):
        pieces = part.reshape(z_size, xc_size, rows, unit).transpose(1, 0, 2, 3)
        pieces = pieces.reshape(xc_size * z_size * rows, unit)
        pieces = lax.psum_scatter(pieces, "xc", scatter_dimension=0, tiled=True)
        pieces = pieces.reshape(z_size, rows, unit)
        pieces = lax.all_to_all(pieces, "z", split_axis=0, concat_axis=0, tiled=True)
        return pieces.transpose(1, 0, 2).reshape(rows, z_size * unit).astype(jnp.float32)

    w_gate_grad, w_up_grad, w_down_grad = [collect(part) for part in weight_parts]

    norm_pull_two = jax.vjp(norm_gain, mid, gain_two)[1]
    grad_mid_norm, grad_gain_two = norm_pull_two(grad_normed_two)
    grad_mid = cotangent.astype(jnp.float32) + grad_mid_norm
    grad_mid_all = lax.all_gather(grad_mid.astype(jnp.bfloat16), "mp", axis=0, tiled=True)
    grad_vals = (
        jnp.dot(grad_mid_all, out_weight, preferred_element_type=jnp.float32)
        .astype(jnp.bfloat16)
        .reshape(seq_len, heads_here, head_dim)
    )
    grad_probs = jnp.einsum("thd,sd->hts", grad_vals, values, preferred_element_type=jnp.float32)
    delta = jnp.sum(probs * grad_probs, axis=-1, keepdims=True)
    grad_scores = (probs * (grad_probs - delta)).astype(jnp.bfloat16)
    grad_rot = jnp.einsum("hts,sd->thd", grad_scores, keys, preferred_element_type=jnp.float32)
    key_sum = jnp.einsum("hts,thd->sd", grad_scores, rotated, preferred_element_type=jnp.float32)
    value_sum = jnp.einsum("hts,thd->sd", probs_low, grad_vals, preferred_element_type=jnp.float32)
    grad_query = (
        (unrotate(grad_rot, cosine[:, None], sine[:, None]) * scale)
        .reshape(seq_len, heads_here * head_dim)
        .astype(jnp.bfloat16)
    )
    grad_kv = jnp.concatenate([unrotate(key_sum, cosine, sine), value_sum], axis=1).astype(
        jnp.bfloat16
    )
    grad_normed_one = lax.psum_scatter(
        (matmul_nt(grad_query, query_weight) + matmul_nt(grad_kv, kv_weight)).astype(jnp.bfloat16),
        "mp",
        scatter_dimension=0,
        tiled=True,
    ).astype(jnp.float32)
    norm_pull_one = jax.vjp(norm_gain, inputs_f, gain_one)[1]
    grad_input_norm, grad_gain_one = norm_pull_one(grad_normed_one)
    tokens_grad = (grad_mid + grad_input_norm).astype(jnp.bfloat16)

    w_query_grad = lax.psum_scatter(
        matmul_tn(normed_one, grad_query).astype(jnp.bfloat16), dp, scatter_dimension=0, tiled=True
    ).astype(jnp.float32)
    w_out_grad = lax.psum_scatter(
        matmul_tn(grad_mid_all, attn_vals).astype(jnp.bfloat16), dp, scatter_dimension=0, tiled=True
    ).astype(jnp.float32)
    small = jnp.concatenate(
        [matmul_tn(normed_one, grad_kv), grad_gain_one[:, None], grad_gain_two[:, None]], axis=1
    )
    small = lax.psum_scatter(small, everywhere, scatter_dimension=0, tiled=True)
    kv_grad = small[:, : 2 * head_dim]
    return (
        mixed,
        tokens_grad,
        small[:, 2 * head_dim],
        small[:, 2 * head_dim + 1],
        kv_grad,
        w_query_grad,
        w_out_grad,
        w_gate_grad,
        w_up_grad,
        w_down_grad,
    )


def shards_fast(
    tokens,
    segments,
    positions,
    cotangent,
    attn_gain,
    ffn_gain,
    w_kv,
    w_query,
    w_out,
    w_gate,
    w_up,
    w_down,
):
    quarter = w_kv.shape[1] // 8
    lane = jnp.arange(2 * quarter)
    freqs = rope_base ** (-(lane % quarter).astype(jnp.float32) / quarter)
    phase = positions.astype(jnp.float32)[:, None] * freqs[None, :]
    table = (jnp.cos(phase), jnp.where(lane < quarter, -1.0, 1.0)[None, :] * jnp.sin(phase))
    (
        normed_one,
        rotated,
        keys,
        values,
        attn_vals,
        mid,
        normed_two,
        gains,
        allowed,
        kv_weight,
        query_weight,
        out_weight,
        ffn_weights,
        grad_all,
    ) = pre_call(
        tokens,
        w_kv,
        attn_gain[None, :],
        ffn_gain[None, :],
        table,
        segments[None, :],
        cotangent,
        w_query,
        w_out,
        (w_gate, w_up, w_down),
    )
    main = ragged_split(w_gate.shape[1], lax.axis_size("z"))[0]
    grad_mid, gain_part, mix_parts, ffn_sums, grad_mid_low = ffn_call(
        gains, normed_two, grad_all, ffn_weights, mid, w_gate.shape[0], main
    )
    mixed, tokens_grad, gain_grads, kv_grad, query_grad, out_grad, ffn_grads = post_call(
        tokens,
        gains,
        gain_part,
        normed_one,
        rotated,
        keys,
        values,
        attn_vals,
        table,
        allowed,
        kv_weight,
        query_weight,
        out_weight,
        mix_parts,
        grad_mid,
        grad_mid_low,
        mid,
        ffn_sums,
        main,
    )
    *ffn_out, query_grad, out_grad, kv_grad, mixed, tokens_grad = layout_call(
        ffn_sums,
        ffn_grads,
        query_grad,
        out_grad,
        kv_grad,
        mixed,
        tokens_grad,
        w_gate.shape[1],
    )
    share = attn_gain.shape[0]
    place = lax.axis_index(("z", "x", "c", "mp")) * share
    gain_grads = gain_grads.reshape(2, gain_grads.size // 2)
    gain_grads = lax.dynamic_slice(gain_grads, (0, place), (2, share))
    return (
        mixed,
        tokens_grad,
        gain_grads[0],
        gain_grads[1],
        kv_grad,
        query_grad,
        out_grad,
        *ffn_out,
    )


def solution(mesh):
    dp_size, mp_size = mesh.shape["dp"], mesh.shape["mp"]
    if dp_size == 4 * FF_SPLIT and mp_size == 2:
        body, dp = shards_fast, ("z", "x", "c")
        sizes = (FF_SPLIT, 2, 2, mp_size)
    else:
        body, dp = shards_general, ("z", "xc")
        sizes = (FF_SPLIT, dp_size // FF_SPLIT, mp_size)
    all_axes = (*dp, "mp")
    fine = jax.sharding.Mesh(mesh.devices.reshape(sizes), all_axes)
    in_specs = (
        P(all_axes, None),
        P(dp),
        P(dp),
        P(all_axes, None),
        P(all_axes),
        P(all_axes),
        P(all_axes, None),
        P(dp, "mp"),
        P(dp, "mp"),
        P(dp, "mp"),
        P(dp, "mp"),
        P(dp, "mp"),
    )
    out_specs = (
        P(all_axes, None),
        P(all_axes, None),
        P(all_axes),
        P(all_axes),
        P(all_axes, None),
        P(dp, "mp"),
        P(dp, "mp"),
        P(dp, "mp"),
        P(dp, "mp"),
        P(dp, "mp"),
    )
    return jax.shard_map(body, mesh=fine, in_specs=in_specs, out_specs=out_specs, check_vma=False)
```

```python
import functools

import jax
import jax.numpy as jnp
from jax import lax
from jax.experimental import pallas as pl
from jax.experimental.pallas import tpu as pltpu
from jax.sharding import PartitionSpec as P

WINDOW = 2048


epsilon = 1e-06
rope_base = 10000.0
masked_score = -1e30
VMEM_BYTES = 66_000_000


def norm_gain(values, gain):
    return values * lax.rsqrt(jnp.mean(values * values, axis=-1, keepdims=True) + epsilon) * gain


def rotary_angles(positions, head_width):
    quarter = head_width // 4
    freqs = rope_base ** (-jnp.arange(quarter).astype(jnp.float32) / quarter)
    phase = positions.astype(jnp.float32)[:, None] * freqs[None, :]
    return (jnp.cos(phase), jnp.sin(phase))


def rotate(values, cosine, sine):
    quarter = cosine.shape[-1]
    first_half = values[..., :quarter]
    second_half = values[..., quarter : 2 * quarter]
    return jnp.concatenate(
        [
            first_half * cosine - second_half * sine,
            second_half * cosine + first_half * sine,
            values[..., 2 * quarter :],
        ],
        axis=-1,
    )


def unrotate(values, cosine, sine):
    quarter = cosine.shape[-1]
    first_half = values[..., :quarter]
    second_half = values[..., quarter : 2 * quarter]
    return jnp.concatenate(
        [
            first_half * cosine + second_half * sine,
            second_half * cosine - first_half * sine,
            values[..., 2 * quarter :],
        ],
        axis=-1,
    )


def gelu_product(gate, up_proj):
    return jax.nn.gelu(gate, approximate=True) * up_proj


def matmul_nt(left, right):
    return lax.dot_general(
        left, right, (((1,), (1,)), ((), ())), preferred_element_type=jnp.float32
    )


def matmul_tn(left, right):
    return lax.dot_general(
        left, right, (((0,), (0,)), ((), ())), preferred_element_type=jnp.float32
    )


def block_allowed(segments, first_row, rows):
    seq_len = segments.shape[0]
    query_rows = first_row + jnp.arange(rows)
    key_rows = jnp.arange(seq_len)
    return (
        (segments[:, None] == segments[None, :])
        & (key_rows[None, :] <= query_rows[:, None])
        & (query_rows[:, None] - key_rows[None, :] < WINDOW)
    )


MESH_ID = pl.DeviceIdType.MESH
GELU_A = 0.7978845608028654
GELU_B = 0.044715
TILE = 256
WIDE = 512


def remote(src, dst, send_sem, recv_sem, where):
    return pltpu.make_async_remote_copy(
        src_ref=src,
        dst_ref=dst,
        send_sem=send_sem,
        recv_sem=recv_sem,
        device_id=where,
        device_id_type=MESH_ID,
    )


class Halves:
    def __init__(self, src, dst, send_sem, recv_sem, where):
        rows = src.shape[0] // 2
        cuts = [pl.ds(part * rows, rows) for part in range(2)]
        self.copies = [
            remote(src.at[cut], dst.at[cut], send_sem.at[part], recv_sem.at[part], where)
            for part, cut in enumerate(cuts)
        ]

    def start(self):
        for copy in self.copies:
            copy.start()

    def wait_recv(self):
        for copy in self.copies:
            copy.wait_recv()

    def wait_send(self):
        for copy in self.copies:
            copy.wait_send()


def dot_nn(left, right):
    return lax.dot_general(
        left, right, (((1,), (0,)), ((), ())), preferred_element_type=jnp.float32
    )


def gelu_parts(gate):
    square = gate * gate
    bend = jnp.tanh(GELU_A * gate * (1.0 + GELU_B * square))
    half = 0.5 * (1.0 + bend)
    slope = half + 0.5 * gate * (1.0 - bend * bend) * GELU_A * (1.0 + 3.0 * GELU_B * square)
    return gate * half, slope


def add_rows(first, rest, out, count):
    def body(index, carry):
        step = pl.ds(pl.multiple_of(index * 32, 32), 32)
        total = first[step, :].astype(jnp.float32)
        for other in rest:
            total = total + other[step, :].astype(jnp.float32)
        out[step, :] = total.astype(out.dtype)
        return carry

    lax.fori_loop(0, count // 32, body, 0)


def norm_back(values, gain, upstream):
    scale = lax.rsqrt(jnp.mean(values * values, axis=-1, keepdims=True) + epsilon)
    normed = values * scale
    pulled = gain * upstream
    back = scale * (pulled - normed * jnp.mean(normed * pulled, axis=-1, keepdims=True))
    return back, jnp.sum(upstream * normed, axis=0, keepdims=True)


def ffn_kernel(
    z_size,
    main,
    gain_ref,
    own_hbm,
    dy_hbm,
    w_hbm,
    mid_hbm,
    gm_ref,
    gain_part,
    mix_hbm,
    sums_hbm,
    gm_hbm,
    n2,
    dy,
    w3,
    h3,
    n2_t,
    dy_t,
    gn_part,
    mix_buf,
    gn_y,
    gn_z,
    gn_s,
    c_in,
    x_in,
    mid,
    load_sem,
    mix_sem,
    ag_y_send,
    ag_y_recv,
    ag_z_send,
    ag_z_recv,
    rs_y_send,
    rs_y_recv,
    rs_z_send,
    rs_z_recv,
    c_send,
    c_recv,
    x_send,
    x_recv,
    out_sem,
):
    own = own_hbm.shape[0] // 2
    width = own_hbm.shape[1]
    units = w3.shape[2]
    rows = c_in.shape[3]
    span = width // z_size
    me_y, me_z = lax.axis_index("mp"), lax.axis_index("z")
    me_x, me_c = lax.axis_index("x"), lax.axis_index("c")
    mine = pl.ds(pl.multiple_of(me_y * own, own), own)
    theirs = pl.ds(pl.multiple_of((1 - me_y) * own, own), own)
    to_y, to_x, to_c = {"mp": 1 - me_y}, {"x": 1 - me_x}, {"c": 1 - me_c}

    def ahead(step):
        return lax.rem(me_z + step, z_size)

    def to_z(step):
        return {"z": ahead(step)}

    def row_block(z_at, x_at, c_at):
        return pl.ds(pl.multiple_of(((z_at * 2 + x_at) * 2 + c_at) * rows, rows), rows)

    inner = (me_z > 0) & (me_z < z_size - 1)
    outer = (me_z == 0) | (me_z == z_size - 1)

    def w_load(index, columns):
        cols = pl.ds(0, columns)
        return pltpu.make_async_copy(
            w_hbm.at[index, :, cols], w3.at[index, :, cols], load_sem.at[z_size + index]
        )

    def w_loads(act):
        for case, columns in ((inner, units), (outer, main)):

            @pl.when(case)
            def _(columns=columns):
                for index in range(3):
                    act(w_load(index, columns))

    w_loads(lambda copy: copy.start())
    dy_loads = [
        pltpu.make_async_copy(dy_hbm.at[index], dy, load_sem.at[index])
        for index in range(z_size)
    ]
    own_load = pltpu.make_async_copy(own_hbm, n2.at[0], load_sem.at[z_size + 3])
    mid_load = pltpu.make_async_copy(mid_hbm, mid, load_sem.at[z_size + 4])
    for load in (own_load, dy_loads[0], mid_load):
        load.start()

    barrier = pltpu.get_barrier_semaphore()
    peers = [to_y, to_x, to_c] + [to_z(step) for step in range(1, z_size)]
    for where in peers:
        pl.semaphore_signal(barrier, inc=1, device_id=where, device_id_type=MESH_ID)
    pl.semaphore_wait(barrier, len(peers))

    def ag_y(index):
        block = n2.at[index, mine]
        return Halves(block, block, ag_y_send.at[index], ag_y_recv.at[index], to_y)

    def ag_y_in(index):
        block = n2.at[index, theirs]
        return Halves(block, block, ag_y_send.at[index], ag_y_recv.at[index], to_y)

    def ag_z(index):
        src = own_hbm.at[mine] if index == 0 else n2.at[index, mine]
        return Halves(
            src, n2.at[index + 1, mine], ag_z_send.at[index], ag_z_recv.at[index + 1], to_z(1)
        )

    def ag_z_in(index):
        block = n2.at[index, mine]
        return Halves(block, block, ag_z_send.at[0], ag_z_recv.at[index], to_z(1))

    def ag_last():
        return Halves(
            n2.at[2, theirs], n2.at[3, theirs], ag_y_send.at[3], ag_y_recv.at[3], to_z(1)
        )

    def forward(index):
        ag_z_in(index).wait_recv()
        ag_z(index).start()
        ag_y(index).start()

    ag_z(0).start()

    mix_copies = []

    def turn(source, target, index):
        def turn_tile(tile, carry):
            at = pl.ds(pl.multiple_of(tile * span, 128), span)
            target[at, pl.ds(index * 2 * own, 2 * own)] = source[:, at].T
            return carry

        lax.fori_loop(0, z_size, turn_tile, 0)

    def chunk(index):
        if index:
            mix_copies[index - 1].wait()
        dy_loads[index].wait()
        rows_at = pl.ds(index * 2 * own, 2 * own)

        def up_tile(tile, carry):
            cols = pl.ds(pl.multiple_of(tile * WIDE, WIDE), WIDE)
            gate = dot_nn(n2[index], w3[0, :, cols])
            up_proj = dot_nn(n2[index], w3[1, :, cols])
            grad_hidden = dot_nn(dy[...], w3[2, :, cols])
            act, slope = gelu_parts(gate)
            h3[0, rows_at, cols] = (grad_hidden * up_proj * slope).astype(jnp.bfloat16)
            h3[1, rows_at, cols] = (grad_hidden * act).astype(jnp.bfloat16)
            h3[2, rows_at, cols] = (act * up_proj).astype(jnp.bfloat16)
            return carry

        lax.fori_loop(0, units // WIDE, up_tile, 0)

        def down_tile(tile, carry):
            at = pl.ds(pl.multiple_of(tile * span, 128), span)
            normed = matmul_nt(w3[0, at, :], h3[0, rows_at, :]) + matmul_nt(
                w3[1, at, :], h3[1, rows_at, :]
            )
            mixed = matmul_nt(w3[2, at, :], h3[2, rows_at, :])
            for half in range(2):
                cols = slice(half * own, (half + 1) * own)
                gn_part[index, half, at, :] = normed[:, cols].astype(jnp.bfloat16)
                mix_buf[half, at, :] = mixed[:, cols].astype(jnp.bfloat16)
            return carry

        lax.fori_loop(0, z_size, down_tile, 0)
        copy = pltpu.make_async_copy(mix_buf, mix_hbm.at[index], mix_sem.at[index])
        copy.start()
        mix_copies.append(copy)
        if index:
            rs_y(index).start()
        turn(n2.at[index], n2_t, index)
        turn(dy, dy_t, index)
        if index + 1 < z_size:
            dy_loads[index + 1].start()

    def rs_y(index):
        return Halves(
            gn_part.at[index, 1 - me_y], gn_y.at[index], rs_y_send.at[index], rs_y_recv.at[index], to_y
        )

    def rs_z(index):
        return Halves(
            gn_s.at[index - 1],
            gn_z.at[index - 1],
            rs_z_send.at[index],
            rs_z_recv.at[index - 1],
            to_z(1),
        )

    def rs_step(index):
        rs_y(index).wait_recv()
        slot = (index - 2) % z_size
        if index != 1:
            Halves(
                gn_s.at[slot], gn_z.at[slot], rs_z_send.at[1], rs_z_recv.at[slot], to_z(1)
            ).wait_recv()

        def add_tile(tile, carry):
            at = pl.ds(pl.multiple_of(tile * TILE, TILE), TILE)
            total = gn_part[index, me_y, at, :].astype(jnp.float32) + gn_y[index, at, :].astype(
                jnp.float32
            )
            if index != 1:
                total = total + gn_z[slot, at, :].astype(jnp.float32)
            if index == 0:
                gm_ref[:, at] = total.T
            else:
                gn_s[index - 1, at, :] = total.astype(jnp.bfloat16)
            return carry

        lax.fori_loop(0, width // TILE, add_tile, 0)
        if index != 0:
            rs_z(index).start()


    def grads(step):
        at = pl.ds(pl.multiple_of(ahead(step) * span, 128), span)
        for kind, source in enumerate((n2_t, n2_t, dy_t)):

            def tile_body(tile, carry, kind=kind, source=source):
                cols = pl.ds(pl.multiple_of(tile * WIDE, WIDE), WIDE)
                w3[kind, at, cols] = dot_nn(source[at, :], h3[kind, :, cols]).astype(jnp.bfloat16)
                return carry

            lax.fori_loop(0, units // WIDE, tile_body, 0)
            for far in (1, 0):
                over_c(kind, step, far).start()

    def over_c(kind, step, far):
        x_at = 1 - me_x if far else me_x
        return remote(
            w3.at[kind, row_block(ahead(step), x_at, 1 - me_c)],
            c_in.at[kind, step, far],
            c_send.at[kind, step, far],
            c_recv.at[kind, step, far],
            to_c,
        )

    def over_x(kind):
        return remote(
            w3.at[kind, row_block(ahead(1), 1 - me_x, me_c)],
            x_in.at[kind],
            x_send.at[kind],
            x_recv.at[kind],
            to_x,
        )

    out_copies = []

    def keep(kind, step, far, block):
        copy = pltpu.make_async_copy(
            block, sums_hbm.at[kind, step, far], out_sem.at[kind, step, far]
        )
        copy.start()
        out_copies.append(copy)

    def core_sums(step):
        pairs = [(kind, far) for kind in range(3) for far in (1, 0)]
        if step == 1:
            pairs.sort(key=lambda pair: -pair[1])
        for kind, far in pairs:
            over_c(kind, step, far).wait_recv()
            x_at = 1 - me_x if far else me_x
            block = w3.at[kind, row_block(ahead(step), x_at, me_c)]
            add_rows(block, [c_in.at[kind, step, far]], block, rows)
            if step != 1:
                keep(kind, step, far, block)
            elif far:
                over_x(kind).start()

    def first_sums():
        for kind in range(3):
            over_x(kind).wait_recv()
            block = w3.at[kind, row_block(ahead(1), me_x, me_c)]
            add_rows(block, [x_in.at[kind]], block, rows)
            keep(kind, 1, 0, block)

    own_load.wait()
    w_loads(lambda copy: copy.wait())

    @pl.when(outer)
    def _():
        w3[:, :, main:] = jnp.zeros((3, width, units - main), jnp.bfloat16)

    chunk(0)
    forward(1)
    forward(2)
    ag_y_in(1).wait_recv()
    chunk(1)
    ag_y_in(2).wait_recv()
    ag_last().start()
    chunk(2)
    rs_step(1)
    ag_z_in(3).wait_recv()
    ag_last().wait_recv()
    chunk(3)
    rs_y(0).start()
    rs_step(2)
    grads(1)
    grads(2)
    core_sums(1)
    rs_step(3)
    grads(3)
    core_sums(2)
    grads(0)
    core_sums(3)
    rs_step(0)
    core_sums(0)

    cot_load = pltpu.make_async_copy(
        dy_hbm.at[0, mine], dy.at[pl.ds(0, own)], load_sem.at[z_size + 3]
    )
    cot_load.start()
    cot_load.wait()
    mid_load.wait()

    def mid_rows(index, total):
        at = pl.ds(pl.multiple_of(index * 32, 32), 32)
        grad, gain_sum = norm_back(mid[at, :], gain_ref[1:2, :], gm_ref[at, :])
        grad = grad + dy[at, :].astype(jnp.float32)
        gm_ref[at, :] = grad
        dy[pl.ds(pl.multiple_of(own + index * 32, 32), 32), :] = grad.astype(jnp.bfloat16)
        return total + gain_sum

    gain_sum = lax.fori_loop(0, own // 32, mid_rows, jnp.zeros((1, width), jnp.float32))
    gm_save = pltpu.make_async_copy(dy.at[pl.ds(own, own)], gm_hbm, load_sem.at[z_size + 3])
    gm_save.start()
    for index in range(4):
        gain_part[index : index + 1, :] = jnp.zeros((1, span), jnp.float32)
        gain_part[4 + index : 5 + index, :] = gain_sum[:, index * span : (index + 1) * span]
    first_sums()
    gm_save.wait()

    for copy in mix_copies[3:] + out_copies:
        copy.wait()
    for index in range(z_size):
        if index in (1, 2):
            ag_y(index).wait_send()
        if index == 3:
            ag_last().wait_send()
        rs_y(index).wait_send()
        if index < z_size - 1:
            ag_z(index).wait_send()
        if index:
            rs_z(index).wait_send()
        for kind in range(3):
            over_c(kind, index, 0).wait_send()
            over_c(kind, index, 1).wait_send()
            if index == 1:
                over_x(kind).wait_send()


def ffn_call(gains, normed, grad_all, weights, mid, rows, main):
    z_size = lax.axis_size("z")
    pair, width = normed.shape
    units = weights.shape[2]
    own = pair // 2
    wide = lambda *lead: pltpu.VMEM((*lead, width), jnp.bfloat16)
    tall = lambda *lead: pltpu.VMEM((*lead, width, own), jnp.bfloat16)
    dma = lambda *lead: pltpu.SemaphoreType.DMA(lead)
    vmem = pl.BlockSpec(memory_space=pltpu.VMEM)
    hbm = pl.BlockSpec(memory_space=pl.ANY)
    return pl.pallas_call(
        functools.partial(ffn_kernel, z_size, main),
        out_shape=(
            jax.ShapeDtypeStruct((own, width), jnp.float32),
            jax.ShapeDtypeStruct((8, width // z_size), jnp.float32),
            jax.ShapeDtypeStruct((z_size, 2, width, own), jnp.bfloat16),
            jax.ShapeDtypeStruct((3, z_size, 2, rows, units), jnp.bfloat16),
            jax.ShapeDtypeStruct((own, width), jnp.bfloat16),
        ),
        in_specs=[vmem, hbm, hbm, hbm, hbm],
        out_specs=(vmem, vmem, hbm, hbm, hbm),
        scratch_shapes=[
            wide(z_size, pair),
            wide(pair),
            pltpu.VMEM(weights.shape, jnp.bfloat16),
            pltpu.VMEM((3, z_size * pair, units), jnp.bfloat16),
            pltpu.VMEM((width, z_size * pair), jnp.bfloat16),
            pltpu.VMEM((width, z_size * pair), jnp.bfloat16),
            tall(z_size, 2),
            tall(2),
            tall(z_size),
            tall(z_size - 1),
            tall(z_size - 1),
            pltpu.VMEM((3, z_size, 2, rows, units), jnp.bfloat16),
            pltpu.VMEM((3, rows, units), jnp.bfloat16),
            pltpu.VMEM((own, width), jnp.float32),
            dma(z_size + 5),
            dma(z_size),
            dma(z_size, 2),
            dma(z_size, 2),
            dma(z_size, 2),
            dma(z_size, 2),
            dma(z_size, 2),
            dma(z_size, 2),
            dma(z_size, 2),
            dma(z_size, 2),
            dma(3, z_size, 2),
            dma(3, z_size, 2),
            dma(3),
            dma(3),
            dma(3, z_size, 2),
        ],
        compiler_params=pltpu.CompilerParams(
            collective_id=0, has_side_effects=True, vmem_limit_bytes=VMEM_BYTES
        ),
        cost_estimate=pl.CostEstimate(
            flops=18 * z_size * pair * width * units,
            bytes_accessed=4 * weights.size + 12 * z_size * pair * width,
            transcendentals=z_size * pair * units,
        ),
    )(gains, normed, grad_all, weights, mid)


def spin(values, table):
    first = values[:, : values.shape[1] // 2]
    turned = first * table[0] + pltpu.roll(first, first.shape[1] // 2, 1) * table[1]
    return jnp.concatenate([turned, values[:, values.shape[1] // 2 :]], axis=1)


def spin_back(values, table):
    first = values[:, : values.shape[1] // 2]
    turned = first * table[0] - pltpu.roll(first, first.shape[1] // 2, 1) * table[1]
    return jnp.concatenate([turned, values[:, values.shape[1] // 2 :]], axis=1)


def head_probs(rotated, keys, allowed):
    scores = jnp.where(allowed > 0.5, matmul_nt(rotated, keys), masked_score)
    weights = jnp.exp(scores - jnp.max(scores, axis=-1, keepdims=True))
    return weights / jnp.sum(weights, axis=-1, keepdims=True)


def ragged_split(columns, parts):
    main = columns // parts // 128 * 128
    return main, main + 128


def pre_kernel(
    z_size,
    tok_ref,
    wkv_ref,
    gain_one_ref,
    gain_two_ref,
    cos_ref,
    sin_ref,
    seg_ref,
    cot_hbm,
    wq_hbm,
    wo_hbm,
    wg_hbm,
    wu_hbm,
    wd_hbm,
    n1_ref,
    rot_ref,
    key_ref,
    val_ref,
    att_ref,
    mid_ref,
    n2_ref,
    gain_ref,
    allow_ref,
    kv_out,
    wq_out,
    wo_out,
    w3_out,
    dy_out,
    kv_w,
    q_w,
    o_w,
    tok,
    part,
    part_y,
    query,
    gain_rows,
    y_send,
    y_recv,
    ky_send,
    ky_recv,
    az_send,
    az_recv,
    ax_send,
    ax_recv,
    ac_send,
    ac_recv,
    fz_send,
    fz_recv,
    fx_send,
    fx_recv,
    fc_send,
    fc_recv,
    dz_send,
    dz_recv,
    dy_send,
    dy_recv,
    local_sem,
):
    me_z, me_x = lax.axis_index("z"), lax.axis_index("x")
    me_c, me_y = lax.axis_index("c"), lax.axis_index("mp")
    own, width = tok_ref.shape
    rows = wq_hbm.shape[0]
    half_rows = wkv_ref.shape[0]
    head = key_ref.shape[1]
    main, units = ragged_split(wg_hbm.shape[1], z_size)
    to_y, to_x, to_c = {"mp": 1 - me_y}, {"x": 1 - me_x}, {"c": 1 - me_c}

    def to_z(step):
        return {"z": lax.rem(me_z + step, z_size)}

    def from_z(step):
        return lax.rem(me_z - step + z_size, z_size)

    def row_block(step, x_at, c_at):
        start = ((from_z(step) * 2 + x_at) * 2 + c_at) * rows
        return pl.ds(pl.multiple_of(start, rows), rows)

    mine = pl.ds(pl.multiple_of(me_y * own, own), own)
    theirs = pl.ds(pl.multiple_of((1 - me_y) * own, own), own)
    bufs = (kv_w, q_w, o_w)
    inputs = (None, wq_hbm, wo_hbm)

    locals_ = []

    def local(src, dst):
        copy = pltpu.make_async_copy(src, dst, local_sem.at[len(locals_)])
        copy.start()
        locals_.append(copy)
        return copy

    here = row_block(0, me_x, me_c)
    own_q = local(wq_hbm, q_w.at[here])
    own_o = local(wo_hbm, o_w.at[here])
    ffn_in = (wg_hbm, wu_hbm, wd_hbm)

    def body_of(target):
        return pl.ds(pl.multiple_of(target * main, 128), main), pl.ds(0, main)

    def tail_of(target):
        start = z_size * main + lax.rem(target + 1, 2) * 128
        return pl.ds(pl.multiple_of(start, 128), 128), pl.ds(main, 128)

    def is_inner(at):
        return (at > 0) & (at < z_size - 1)

    own_f = []
    for kind in range(3):
        src, dst = body_of(me_z)
        own_f.append(local(ffn_in[kind].at[:, src], w3_out.at[kind, here, dst]))

    def own_tail(kind):
        src, dst = tail_of(me_z)
        return pltpu.make_async_copy(
            ffn_in[kind].at[:, src], w3_out.at[kind, here, dst], local_sem.at[12 + kind]
        )

    @pl.when(is_inner(me_z))
    def _():
        for kind in range(3):
            own_tail(kind).start()
    own_d = local(cot_hbm, dy_out.at[0, mine])

    kv_own = pl.ds(pl.multiple_of(here.start + me_y * half_rows, half_rows), half_rows)
    gain_rows[...] = jnp.zeros(gain_rows.shape, jnp.float32)
    gain_rows[0:1, :half_rows] = gain_one_ref[...].astype(jnp.float32)
    gain_rows[1:2, :half_rows] = gain_two_ref[...].astype(jnp.float32)
    spread = gain_rows[...].T
    kv_w[kv_own, : 2 * head] = wkv_ref[...]
    kv_w[kv_own, 2 * head :] = spread[:half_rows, :].astype(jnp.bfloat16)

    barrier = pltpu.get_barrier_semaphore()
    peers = [to_y, to_x, to_c] + [to_z(step) for step in range(1, z_size)]
    for where in peers:
        pl.semaphore_signal(barrier, inc=1, device_id=where, device_id_type=MESH_ID)
    pl.semaphore_wait(barrier, len(peers))

    tok_y = remote(tok_ref, tok.at[mine], y_send.at[1], y_recv.at[1], to_y)
    tok_y_in = remote(tok_ref, tok.at[theirs], y_send.at[1], y_recv.at[1], to_y)
    part_out = remote(part.at[theirs], part_y, y_send.at[2], y_recv.at[2], to_y)
    n2_y = remote(n2_ref.at[mine], n2_ref.at[mine], y_send.at[3], y_recv.at[3], to_y)
    n2_y_in = remote(n2_ref.at[theirs], n2_ref.at[theirs], y_send.at[3], y_recv.at[3], to_y)

    def block_of(kind, step, x_at):
        if kind:
            return row_block(step, x_at, me_c)
        return kv_rows(step, x_at, me_y)

    def kv_rows(step, x_at, y_at):
        start = row_block(step, x_at, me_c).start + y_at * half_rows
        return pl.ds(pl.multiple_of(start, half_rows), half_rows)

    def kv_y(step, far):
        x_at = 1 - me_x if far else me_x
        block = kv_w.at[kv_rows(step, x_at, me_y)]
        slot = step + z_size * far
        return remote(block, block, ky_send.at[slot], ky_recv.at[slot], to_y)

    def kv_y_in(step, far):
        x_at = 1 - me_x if far else me_x
        block = kv_w.at[kv_rows(step, x_at, 1 - me_y)]
        slot = step + z_size * far
        return remote(block, block, ky_send.at[slot], ky_recv.at[slot], to_y)

    def source(kind, step):
        if isinstance(step, int) and step == 0 and kind:
            return inputs[kind]
        return bufs[kind].at[block_of(kind, step, me_x)]

    first_z, last_z = (z_size - 1 - me_z) // (z_size - 1), me_z // (z_size - 1)
    inner = first_z + last_z == 0
    order = (0, 1 + 2 * first_z, 3 - first_z - last_z, 2 - first_z + last_z)
    hops = (
        None,
        (lax.rem(me_z + 1, z_size), 2),
        (lax.rem(me_z + z_size - 1, z_size), 2),
        (lax.rem(3 * (me_z + 3), z_size), lax.rem(2 * me_z + 3, z_size)),
    )

    def a_z_own(kind, right):
        return remote(
            source(kind, 0),
            bufs[kind].at[block_of(kind, 0, me_x)],
            az_send.at[kind, right],
            az_recv.at[kind, 1 if right else z_size - 1],
            to_z(1 if right else z_size - 1),
        )

    def a_z_start(kind):
        @pl.when(last_z == 0)
        def _():
            a_z_own(kind, 1).start()

        @pl.when(first_z == 0)
        def _():
            a_z_own(kind, 0).start()

    def a_z(kind, index):
        target, slot = hops[index]
        block = bufs[kind].at[block_of(kind, order[index], me_x)]
        return remote(
            block, block, az_send.at[kind, 1 + index], az_recv.at[kind, slot], {"z": target}
        )

    def a_z_next(kind, index):
        @pl.when(inner)
        def _():
            a_z(kind, index).start()

    def a_z_done(kind):
        @pl.when(last_z == 0)
        def _():
            a_z_own(kind, 1).wait_send()

        @pl.when(first_z == 0)
        def _():
            a_z_own(kind, 0).wait_send()

        @pl.when(inner)
        def _():
            for index in range(1, z_size):
                a_z(kind, index).wait_send()

    def a_z_in(kind, step):
        block = bufs[kind].at[block_of(kind, step, me_x)]
        return remote(block, block, az_send.at[kind, 0], az_recv.at[kind, step], to_z(1))

    def a_x(kind, step):
        return remote(
            source(kind, step),
            bufs[kind].at[block_of(kind, step, me_x)],
            ax_send.at[kind, step],
            ax_recv.at[kind, step],
            to_x,
        )

    def a_x_in(kind, step):
        block = bufs[kind].at[block_of(kind, step, 1 - me_x)]
        return remote(block, block, ax_send.at[kind, step], ax_recv.at[kind, step], to_x)

    def a_c(kind, step, far):
        x_at = 1 - me_x if far else me_x
        block = bufs[kind].at[row_block(step, x_at, me_c)]
        src = source(kind, step) if kind and not far else block
        slot = step + z_size * far
        return remote(src, block, ac_send.at[kind, slot], ac_recv.at[kind, slot], to_c)

    def a_c_in(kind, step, far):
        x_at = 1 - me_x if far else me_x
        block = bufs[kind].at[row_block(step, x_at, 1 - me_c)]
        slot = step + z_size * far
        return remote(block, block, ac_send.at[kind, slot], ac_recv.at[kind, slot], to_c)

    def f_z(kind, step, act):
        target = lax.rem(me_z + step, z_size)

        def piece(index, src, dst):
            return remote(
                ffn_in[kind].at[:, src],
                w3_out.at[kind, here, dst],
                fz_send.at[kind, step, index],
                fz_recv.at[kind, step, index],
                to_z(step),
            )

        act(piece(0, *body_of(target)))

        @pl.when(is_inner(target))
        def _():
            act(piece(1, *tail_of(target)))

    def f_z_wait(kind, step):
        block = row_block(step, me_x, me_c)

        def piece(index, dst):
            part = w3_out.at[kind, block, dst]
            return remote(
                part, part, fz_send.at[kind, step, index], fz_recv.at[kind, step, index], to_z(step)
            )

        piece(0, pl.ds(0, main)).wait_recv()

        @pl.when(inner)
        def _():
            piece(1, pl.ds(main, 128)).wait_recv()

    def f_x(kind, step, x_at, act):
        for case, columns in ((inner, units), (first_z + last_z > 0, main)):

            @pl.when(case)
            def _(columns=columns):
                block = w3_out.at[kind, row_block(step, x_at, me_c), pl.ds(0, columns)]
                act(remote(block, block, fx_send.at[kind, step], fx_recv.at[kind, step], to_x))

    def f_x_start(kind, step):
        f_x(kind, step, me_x, lambda copy: copy.start())

    def f_x_wait(kind, step):
        f_x(kind, step, 1 - me_x, lambda copy: copy.wait_recv())

    def f_x_done(kind, step):
        f_x(kind, step, me_x, lambda copy: copy.wait_send())

    def f_c(kind, step, far):
        block = w3_out.at[kind, row_block(step, 1 - me_x if far else me_x, me_c)]
        slot = step + z_size * far
        return remote(block, block, fc_send.at[kind, slot], fc_recv.at[kind, slot], to_c)

    def f_c_in(kind, step, far):
        block = w3_out.at[kind, row_block(step, 1 - me_x if far else me_x, 1 - me_c)]
        slot = step + z_size * far
        return remote(block, block, fc_send.at[kind, slot], fc_recv.at[kind, slot], to_c)

    def d_source(step):
        return cot_hbm if isinstance(step, int) else dy_out.at[step, mine]

    def d_z_own(right):
        slot = 1 if right else z_size - 1
        return remote(
            cot_hbm, dy_out.at[slot, mine], dz_send.at[right], dz_recv.at[slot], to_z(slot)
        )

    def d_z(index):
        target, slot = hops[index]
        return remote(
            dy_out.at[order[index], mine],
            dy_out.at[slot, mine],
            dz_send.at[1 + index],
            dz_recv.at[slot],
            {"z": target},
        )

    def d_z_done():
        @pl.when(last_z == 0)
        def _():
            d_z_own(1).wait_send()

        @pl.when(first_z == 0)
        def _():
            d_z_own(0).wait_send()

        @pl.when(inner)
        def _():
            for index in range(1, z_size):
                d_z(index).wait_send()

    def d_z_in(step):
        block = dy_out.at[step, mine]
        return remote(block, block, dz_send.at[0], dz_recv.at[step], to_z(1))

    def d_y(step):
        return remote(
            d_source(step), dy_out.at[step, mine], dy_send.at[step], dy_recv.at[step], to_y
        )

    def d_y_in(step):
        block = dy_out.at[step, theirs]
        return remote(block, block, dy_send.at[step], dy_recv.at[step], to_y)

    for kind in (1, 0, 2):
        a_z_start(kind)
        a_x(kind, 0).start()
    kv_y(0, 0).start()
    tok_y.start()
    for kind in (1, 2):
        a_c(kind, 0, 0).start()

    for at_end, away in ((first_z, 1), (last_z, z_size - 1)):

        @pl.when(at_end > 0)
        def _(away=away):
            d_z_own(1 if away == 1 else 0).start()
            for kind in range(3):
                f_z(kind, away, lambda copy: copy.start())

    tok[mine, :] = tok_ref[...]
    seq = 2 * own
    query_at = lax.broadcasted_iota(jnp.int32, (seq, seq), 0)
    key_at = lax.broadcasted_iota(jnp.int32, (seq, seq), 1)
    segment = seg_ref[...].astype(jnp.float32)
    same = jnp.broadcast_to(segment, (8, seq)).T[:, :1] == segment
    allowed = same & (key_at <= query_at) & (query_at - key_at < WINDOW)
    allow_ref[...] = jnp.where(allowed, 1.0, 0.0)
    d_y(0).start()

    def pass_cotangent(index):
        d_z_in(order[index]).wait_recv()

        @pl.when(inner)
        def _():
            d_z(index).start()

        d_y(order[index]).start()

    def pass_at(at, index):
        @pl.when(me_z == at)
        def _():
            pass_cotangent(index)

    def pass_if(case, index):
        @pl.when(case)
        def _():
            pass_cotangent(index)

    outer = first_z + last_z > 0

    def from_x(index):
        step = order[index]
        for kind in (1, 0, 2):
            a_x_in(kind, step).wait_recv()
            if kind:
                a_c(kind, step, 1).start()
            else:
                kv_y(step, 1).start()

    def from_y(index):
        step = order[index]
        for far in range(2):
            kv_y_in(step, far).wait_recv()
            a_c(0, step, far).start()

    for index in range(1, z_size):
        step = order[index]
        for kind in (1, 0, 2):
            a_z_in(kind, step).wait_recv()
            a_z_next(kind, index)
            a_x(kind, step).start()
            if kind:
                a_c(kind, step, 0).start()
            else:
                kv_y(step, 0).start()
        if index == z_size - 2:

            @pl.when(inner)
            def _():
                d_z_own(1).start()
                d_z_own(0).start()

        if index == z_size - 1:
            pass_at(1, 1)
            pass_at(2, 2)
            for copy in own_f:
                copy.wait()

            @pl.when(inner)
            def _():
                for kind in range(3):
                    own_tail(kind).wait()

            for kind in range(3):
                for away, sent in ((1, first_z), (3, last_z), (2, 0)):

                    @pl.when(sent == 0 if away != 2 else me_z >= 0)
                    def _(kind=kind, away=away):
                        f_z(kind, away, lambda copy: copy.start())

            for kind in range(3):
                f_x_start(kind, 0)
                f_c(kind, 0, 0).start()
        if index >= 2:
            from_x(index - 2)
            from_y(index - 2)
    from_x(z_size - 2)
    from_y(z_size - 2)
    pass_at(1, 2)
    pass_at(2, 1)
    pass_if(outer, 1)
    from_x(z_size - 1)
    from_y(z_size - 1)

    def hand_on(kind, step):
        f_z_wait(kind, step)
        f_x_start(kind, step)
        f_c(kind, step, 0).start()

    def cross(kind, step):
        f_x_wait(kind, step)
        f_c(kind, step, 1).start()

    tok_y_in.wait_recv()
    own_q.wait()
    own_o.wait()
    for kind in (0, 1):
        for step in range(z_size):
            for far in range(2):
                a_c_in(kind, step, far).wait_recv()

    gains = kv_w[:, 2 * head :].astype(jnp.float32).T[:8, :]
    gain_ref[...] = gains

    def norm_rows(index, carry):
        at = pl.ds(pl.multiple_of(index * 32, 32), 32)
        values = tok[at, :].astype(jnp.float32)
        scale = lax.rsqrt(jnp.mean(values * values, axis=-1, keepdims=True) + epsilon)
        n1_ref[at, :] = (values * scale * gain_ref[0:1, :]).astype(jnp.bfloat16)
        return carry

    lax.fori_loop(0, 2 * own // 32, norm_rows, 0)
    pass_if(inner, 3)
    hand_on(0, order[1])
    table = (cos_ref[...], sin_ref[...])
    key_ref[...] = spin(dot_nn(n1_ref[...], kv_w[:, :head]), table).astype(jnp.bfloat16)
    val_ref[...] = dot_nn(n1_ref[...], kv_w[:, head : 2 * head]).astype(jnp.bfloat16)
    hand_on(0, order[2])
    head_scale = head ** (-0.5)
    heads = att_ref.shape[1] // head

    half_cols = att_ref.shape[1] // 2
    for index in range(2):
        cols = pl.ds(index * half_cols, half_cols)
        query[:, cols] = dot_nn(n1_ref[...], q_w[:, cols])

    def attend(index):
        cols = pl.ds(index * head, head)
        rotated = (spin(query[:, cols], table) * head_scale).astype(jnp.bfloat16)
        rot_ref[:, cols] = rotated
        probs = head_probs(rotated, key_ref[...], allow_ref[...]).astype(jnp.bfloat16)
        att_ref[:, cols] = dot_nn(probs, val_ref[...]).astype(jnp.bfloat16)

    tasks = [
        lambda: hand_on(0, order[3]),
        lambda: (cross(0, 0), hand_on(1, order[1])),
        lambda: cross(1, 0),
        lambda: hand_on(1, order[2]),
        lambda: (cross(2, 0), pass_if(outer, 2)),
    ]
    for index in range(heads):
        attend(index)
        if index < len(tasks):
            tasks[index]()
    for step in range(z_size):
        for far in range(2):
            a_c_in(2, step, far).wait_recv()
    saves = [
        local(kv_w, kv_out),
        local(q_w, wq_out),
        local(o_w, wo_out),
    ]
    span = width // 4

    def project(index, carry):
        cols = pl.ds(pl.multiple_of(index * span, span), span)
        part[:, cols] = matmul_nt(att_ref[...], o_w[cols, :]).astype(jnp.bfloat16)
        return carry

    lax.fori_loop(0, 4, project, 0)
    part_out.start()
    hand_on(1, order[3])
    pass_if(outer, 3)
    cross(0, order[1])
    hand_on(2, order[1])
    part_out.wait_recv()

    def middle(index, carry):
        at = pl.ds(pl.multiple_of(index * 32, 32), 32)
        there = pl.ds(pl.multiple_of(me_y * own + index * 32, 32), 32)
        values = (
            tok_ref[at, :].astype(jnp.float32)
            + part[there, :].astype(jnp.float32)
            + part_y[at, :].astype(jnp.float32)
        )
        mid_ref[at, :] = values
        scale = lax.rsqrt(jnp.mean(values * values, axis=-1, keepdims=True) + epsilon)
        n2_ref[there, :] = (values * scale * gain_ref[1:2, :]).astype(jnp.bfloat16)
        return carry

    lax.fori_loop(0, own // 32, middle, 0)
    n2_y.start()
    hand_on(2, order[2])
    cross(0, order[2])
    cross(0, order[3])
    hand_on(2, order[3])
    for kind in (1, 2):
        for index in (1, 2, 3):
            cross(kind, order[index])
    for kind in range(3):
        for step in range(z_size):
            for far in range(2):
                f_c_in(kind, step, far).wait_recv()
    for step in range(z_size):
        d_y_in(step).wait_recv()
    n2_y_in.wait_recv()

    for kind in range(3):
        a_z_done(kind)
    d_z_done()
    tok_y.wait_send()
    part_out.wait_send()
    n2_y.wait_send()
    own_d.wait()
    for copy in saves:
        copy.wait()
    for step in range(z_size):
        d_y(step).wait_send()
        for far in range(2):
            kv_y(step, far).wait_send()
        for kind in range(3):
            if step:
                f_z(kind, step, lambda copy: copy.wait_send())
            a_x(kind, step).wait_send()
            f_x_done(kind, step)
            for far in range(2):
                a_c(kind, step, far).wait_send()
                f_c(kind, step, far).wait_send()


def pre_call(
    tokens, w_kv, gain_one, gain_two, table, segments, cotangent, w_query, w_out, ffn
):
    z_size = lax.axis_size("z")
    own, width = tokens.shape
    seq = 2 * own
    rows, cols = w_query.shape
    head = table[0].shape[1] * 2
    units = ragged_split(ffn[0].shape[1], z_size)[1]
    low = lambda *dims: jax.ShapeDtypeStruct(dims, jnp.bfloat16)
    full = lambda *dims: jax.ShapeDtypeStruct(dims, jnp.float32)
    dma = lambda *lead: pltpu.SemaphoreType.DMA(lead)
    vmem = pl.BlockSpec(memory_space=pltpu.VMEM)
    hbm = pl.BlockSpec(memory_space=pl.ANY)
    wide = lambda *lead: pltpu.VMEM((*lead, width), jnp.bfloat16)
    return pl.pallas_call(
        functools.partial(pre_kernel, z_size),
        out_shape=(
            low(seq, width),
            low(seq, cols),
            low(seq, head),
            low(seq, head),
            low(seq, cols),
            full(own, width),
            low(seq, width),
            full(8, width),
            full(seq, seq),
            low(width, 2 * head + 128),
            low(width, cols),
            low(width, cols),
            low(3, width, units),
            low(z_size, seq, width),
        ),
        in_specs=[vmem] * 7 + [hbm] * 6,
        out_specs=(vmem,) * 9 + (hbm,) * 5,
        scratch_shapes=[
            pltpu.VMEM((width, 2 * head + 128), jnp.bfloat16),
            pltpu.VMEM((width, cols), jnp.bfloat16),
            pltpu.VMEM((width, cols), jnp.bfloat16),
            wide(seq),
            wide(seq),
            wide(own),
            pltpu.VMEM((seq, cols), jnp.float32),
            pltpu.VMEM((128, 128), jnp.float32),
            dma(4),
            dma(4),
            dma(2 * z_size),
            dma(2 * z_size),
            dma(3, z_size + 1),
            dma(3, z_size),
            dma(3, z_size),
            dma(3, z_size),
            dma(3, 2 * z_size),
            dma(3, 2 * z_size),
            dma(3, z_size, 2),
            dma(3, z_size, 2),
            dma(3, z_size),
            dma(3, z_size),
            dma(3, 2 * z_size),
            dma(3, 2 * z_size),
            dma(z_size + 1),
            dma(z_size),
            dma(z_size),
            dma(z_size),
            dma(16),
        ],
        compiler_params=pltpu.CompilerParams(
            collective_id=1, has_side_effects=True, vmem_limit_bytes=VMEM_BYTES
        ),
        cost_estimate=pl.CostEstimate(
            flops=8 * seq * width * cols,
            bytes_accessed=8 * width * (cols + units),
            transcendentals=seq * seq * cols // head,
        ),
    )(tokens, w_kv, gain_one, gain_two, *table, segments, cotangent, w_query, w_out, *ffn)


def post_kernel(
    z_size,
    main,
    tok_ref,
    gain_ref,
    gain_part_ref,
    n1_ref,
    rot_ref,
    key_ref,
    val_ref,
    att_ref,
    cos_ref,
    sin_ref,
    allow_ref,
    kv_hbm,
    wq_hbm,
    wo_hbm,
    mix_hbm,
    gmf_hbm,
    gmb_hbm,
    mid_hbm,
    sums_hbm,
    mixed_ref,
    tgrad_ref,
    gsum_ref,
    kvg_ref,
    qg_ref,
    og_ref,
    ffn_out,
    kv_w,
    q_w,
    o_w,
    o_part,
    gm,
    gm_f,
    gq,
    gkv,
    kv_sum,
    back_y,
    mix_y,
    mix_z,
    mix_s,
    o_c,
    o_x,
    o_z,
    q_c,
    q_x,
    q_z,
    kv_y,
    kv_c,
    kv_x,
    kv_z,
    gain_own,
    gain_in,
    ffn_in,
    ffn_own,
    load_sem,
    own_sem,
    fx_send,
    fx_recv,
    fz_send,
    fz_recv,
    y_send,
    y_recv,
    my_send,
    my_recv,
    mz_send,
    mz_recv,
    wc_send,
    wc_recv,
    wx_send,
    wx_recv,
    wz_send,
    wz_recv,
    kc_send,
    kc_recv,
    kz_send,
    kz_recv,
    g_send,
    g_recv,
):
    me_z, me_x = lax.axis_index("z"), lax.axis_index("x")
    me_c, me_y = lax.axis_index("c"), lax.axis_index("mp")
    own, width = tok_ref.shape
    seq = 2 * own
    head = key_ref.shape[1]
    cols_here = att_ref.shape[1]
    heads = cols_here // head
    rows = qg_ref.shape[0]
    span = width // z_size
    mine = pl.ds(pl.multiple_of(me_y * own, own), own)
    theirs = pl.ds(pl.multiple_of((1 - me_y) * own, own), own)
    to_y, to_x, to_c = {"mp": 1 - me_y}, {"x": 1 - me_x}, {"c": 1 - me_c}
    head_scale = head ** (-0.5)

    def behind(step):
        return lax.rem(me_z - step + z_size, z_size)

    def to_z(step):
        return {"z": lax.rem(me_z + step, z_size)}

    def row_block(step, x_at, c_at):
        start = ((behind(step) * 2 + x_at) * 2 + c_at) * rows
        return pl.ds(pl.multiple_of(start, rows), rows)

    loads = [
        pltpu.make_async_copy(wo_hbm, o_w, load_sem.at[0]),
        pltpu.make_async_copy(wq_hbm, q_w, load_sem.at[1]),
        pltpu.make_async_copy(
            kv_hbm.at[:, :, :, :, :, pl.ds(0, 2 * head)], kv_w, load_sem.at[2]
        ),
    ]
    for step in range(z_size):
        loads.append(
            pltpu.make_async_copy(mix_hbm.at[step, me_y], mix_s.at[step], load_sem.at[3 + step])
        )
    loads.append(pltpu.make_async_copy(gmf_hbm, gm_f, load_sem.at[3 + z_size]))
    loads.append(pltpu.make_async_copy(gmb_hbm, gm.at[mine], load_sem.at[4 + z_size]))
    mid_load = pltpu.make_async_copy(mid_hbm, gm_f, load_sem.at[5 + z_size])
    for load in loads:
        load.start()

    barrier = pltpu.get_barrier_semaphore()
    peers = [to_y, to_x, to_c] + [to_z(step) for step in range(1, z_size)]
    for where in peers:
        pl.semaphore_signal(barrier, inc=1, device_id=where, device_id_type=MESH_ID)
    pl.semaphore_wait(barrier, len(peers))

    tasks = [(step, kind) for step in (2, 3) for kind in range(3)]

    def f_x(index):
        step, kind = tasks[index]
        return remote(
            sums_hbm.at[kind, step, 1],
            ffn_in.at[index],
            fx_send.at[index],
            fx_recv.at[index],
            to_x,
        )

    def f_own(index):
        step, kind = tasks[index]
        return pltpu.make_async_copy(
            sums_hbm.at[kind, step, 0], ffn_own.at[index % 2], own_sem.at[index % 2]
        )

    def f_z(step, kind, source_z, act):
        for case, columns in (
            ((source_z > 0) & (source_z < z_size - 1), ffn_out.shape[3]),
            ((source_z == 0) | (source_z == z_size - 1), main),
        ):

            @pl.when(case)
            def _(columns=columns):
                cols = pl.ds(0, columns)
                if step == 1:
                    src = sums_hbm.at[kind, 1, 0, :, cols]
                else:
                    src = ffn_in.at[tasks.index((step, kind)), :, cols]
                act(
                    remote(
                        src,
                        ffn_out.at[kind, step, :, cols],
                        fz_send.at[kind, step],
                        fz_recv.at[kind, step],
                        to_z(step),
                    )
                )

    def tick(index):
        step, kind = tasks[index]
        f_x(index).wait_recv()
        f_own(index).wait()
        block = ffn_in.at[index]
        add_rows(block, [ffn_own.at[index % 2]], block, rows)
        if index + 2 < len(tasks):
            f_own(index + 2).start()
        f_z(step, kind, me_z, lambda copy: copy.start())

    def f_x_own(kind):
        return remote(
            sums_hbm.at[kind, 0, 1],
            ffn_out.at[kind, 0],
            fx_send.at[len(tasks) + kind],
            fx_recv.at[len(tasks) + kind],
            to_x,
        )

    f_own(0).start()
    f_own(1).start()
    for index in range(len(tasks)):
        f_x(index).start()
    for kind in range(3):
        f_z(1, kind, me_z, lambda copy: copy.start())

    gm_y = remote(gmb_hbm, gm.at[mine], y_send.at[0], y_recv.at[0], to_y)
    gm_y_in = remote(gm.at[theirs], gm.at[theirs], y_send.at[0], y_recv.at[0], to_y)
    gm_y.start()

    first_z, last_z = (z_size - 1 - me_z) // (z_size - 1), me_z // (z_size - 1)
    inner = first_z + last_z == 0
    order = (
        0,
        1 + (me_z + 1) // 2,
        2 + (2 * me_z - 3) * (1 - first_z - last_z),
        3 - 2 * (me_z // 2),
    )
    right = (None, 1 - me_z // 2, (3 - me_z) * (2 - me_z) // 6 + me_z // 2 * (1 - last_z), 1 - me_z // 2)

    def hop_slot(index):
        step, way = order[index], right[index]
        return way * lax.rem(step + 1, z_size) + (1 - way) * (step - 1 + 4 * ((3 - step) // 2))

    def hop_target(index):
        return {"z": me_z + 2 * right[index] - 1}

    def mix_over_y(step):
        return remote(
            mix_hbm.at[step, 1 - me_y], mix_y.at[step], my_send.at[step], my_recv.at[step], to_y
        )

    def mix_over_z(index):
        slot = hop_slot(index)
        return remote(
            mix_s.at[order[index]],
            mix_z.at[slot],
            mz_send.at[index],
            mz_recv.at[slot],
            hop_target(index),
        )

    def mix_z_in(slot):
        return remote(mix_z.at[slot], mix_z.at[slot], mz_send.at[1], mz_recv.at[slot], to_z(1))

    def mix_add(step, others, last):
        def add_tile(tile, carry):
            at = pl.ds(pl.multiple_of(tile * TILE, TILE), TILE)
            total = mix_s[step, at, :].astype(jnp.float32)
            for other in others:
                total = total + other[at, :].astype(jnp.float32)
            if last:
                mixed_ref[:, at] = (gm_f[:, at] + total.T).astype(jnp.bfloat16)
            else:
                mix_s[step, at, :] = total.astype(jnp.bfloat16)
            return carry

        lax.fori_loop(0, width // TILE, add_tile, 0)

    def mix_step(index):
        step = order[index]
        mix_over_y(step).wait_recv()
        from_y = mix_y.at[step]
        if index:

            @pl.when(inner)
            def _():
                mix_z_in(step).wait_recv()
                mix_add(step, [from_y, mix_z.at[step]], False)

            @pl.when(first_z + last_z > 0)
            def _():
                mix_add(step, [from_y], False)

            mix_over_z(index).start()
        else:
            mid_load.wait()

            @pl.when(first_z == 0)
            def _():
                mix_z_in(0).wait_recv()

            @pl.when(last_z == 0)
            def _():
                mix_z_in(z_size).wait_recv()

            @pl.when(inner)
            def _():
                mix_add(0, [from_y, mix_z.at[0], mix_z.at[z_size]], True)

            @pl.when(first_z > 0)
            def _():
                mix_add(0, [from_y, mix_z.at[z_size]], True)

            @pl.when(last_z > 0)
            def _():
                mix_add(0, [from_y, mix_z.at[0]], True)

    for index in (1, 2, 3, 0):
        mix_over_y(order[index]).start()

    kinds = ((o_part, o_c, o_x, o_z, og_ref), (o_w, q_c, q_x, q_z, qg_ref))

    def w_c(kind, step, far):
        x_at = 1 - me_x if far else me_x
        return remote(
            kinds[kind][0].at[row_block(step, x_at, 1 - me_c)],
            kinds[kind][1].at[step, far],
            wc_send.at[kind, step, far],
            wc_recv.at[kind, step, far],
            to_c,
        )

    def w_x(kind, step):
        return remote(
            kinds[kind][0].at[row_block(step, 1 - me_x, me_c)],
            kinds[kind][2].at[step],
            wx_send.at[kind, step],
            wx_recv.at[kind, step],
            to_x,
        )

    def w_z(kind, index):
        step, slot = order[index], hop_slot(index)
        return remote(
            kinds[kind][0].at[row_block(step, me_x, me_c)],
            kinds[kind][3].at[slot],
            wz_send.at[kind, index],
            wz_recv.at[kind, slot],
            hop_target(index),
        )

    def w_z_in(kind, slot):
        block = kinds[kind][3].at[slot]
        return remote(block, block, wz_send.at[kind, 1], wz_recv.at[kind, slot], to_z(1))

    def w_x_stage(kind, index):
        step = order[index]
        w_c(kind, step, 1).wait_recv()
        block = kinds[kind][0].at[row_block(step, 1 - me_x, me_c)]
        add_rows(block, [kinds[kind][1].at[step, 1]], block, rows)
        w_x(kind, step).start()

    def w_z_stage(kind, index):
        part, from_c, from_x, from_z, result = kinds[kind]
        step = order[index]
        w_c(kind, step, 0).wait_recv()
        w_x(kind, step).wait_recv()
        block = part.at[row_block(step, me_x, me_c)]
        others = [from_c.at[step, 0], from_x.at[step]]
        if index:

            @pl.when(inner)
            def _():
                w_z_in(kind, step).wait_recv()
                add_rows(block, [*others, from_z.at[step]], block, rows)

            @pl.when(first_z + last_z > 0)
            def _():
                add_rows(block, others, block, rows)

            w_z(kind, index).start()
        else:

            @pl.when(first_z == 0)
            def _():
                w_z_in(kind, 0).wait_recv()

            @pl.when(last_z == 0)
            def _():
                w_z_in(kind, z_size).wait_recv()

            @pl.when(inner)
            def _():
                add_rows(block, [*others, from_z.at[0], from_z.at[z_size]], result, rows)

            @pl.when(first_z > 0)
            def _():
                add_rows(block, [*others, from_z.at[z_size]], result, rows)

            @pl.when(last_z > 0)
            def _():
                add_rows(block, [*others, from_z.at[0]], result, rows)

    def w_product(kind, index, left, values):
        step = order[index]
        at = pl.ds(pl.multiple_of(behind(step) * span, 128), span)
        turned = left[:, at].T

        def tile_body(tile, carry):
            cols = pl.ds(pl.multiple_of(tile * TILE, TILE), TILE)
            kinds[kind][0][at, cols] = dot_nn(turned, values[:, cols]).astype(jnp.bfloat16)
            return carry

        lax.fori_loop(0, cols_here // TILE, tile_body, 0)
        for far in (1, 0):
            w_c(kind, step, far).start()

    tick(0)
    tick(1)
    loads[-1].wait()
    gm_y_in.wait_recv()
    w_product(0, 1, gm, att_ref)
    w_product(0, 2, gm, att_ref)
    w_x_stage(0, 1)
    w_product(0, 3, gm, att_ref)
    w_x_stage(0, 2)
    tick(2)
    w_product(0, 0, gm, att_ref)
    w_x_stage(0, 3)
    for load in loads[:-1]:
        load.wait()

    kv_sum[...] = jnp.zeros(kv_sum.shape, jnp.float32)
    table = (cos_ref[...], sin_ref[...])

    for index in range(2):
        cols = pl.ds(index * (cols_here // 2), cols_here // 2)
        gq[:, cols] = dot_nn(gm[...], o_w[:, cols]).astype(jnp.bfloat16)

    def attend_back(index):
        cols = pl.ds(index * head, head)
        grad_vals = gq[:, cols]
        rotated = rot_ref[:, cols]
        probs = head_probs(rotated, key_ref[...], allow_ref[...])
        grad_probs = matmul_nt(grad_vals, val_ref[...])
        delta = jnp.sum(probs * grad_probs, axis=-1, keepdims=True)
        grad_scores = (probs * (grad_probs - delta)).astype(jnp.bfloat16)
        grad_rot = dot_nn(grad_scores, key_ref[...])
        gq[:, cols] = (spin_back(grad_rot, table) * head_scale).astype(jnp.bfloat16)
        kv_sum[0] += matmul_tn(grad_scores, rotated)
        kv_sum[1] += matmul_tn(probs.astype(jnp.bfloat16), grad_vals)

    for index in range(heads):
        attend_back(index)
        if index == 0:
            w_x_stage(0, 0)
        if 3 + index < len(tasks):
            tick(3 + index)
        if index == heads - 1:
            mix_step(1)
    gkv[:, :head] = spin_back(kv_sum[0], table).astype(jnp.bfloat16)
    gkv[:, head:] = kv_sum[1].astype(jnp.bfloat16)

    w_product(1, 1, n1_ref, gq)
    w_product(1, 2, n1_ref, gq)
    w_x_stage(1, 1)
    w_z_stage(0, 1)
    w_product(1, 3, n1_ref, gq)
    w_x_stage(1, 2)
    w_product(1, 0, n1_ref, gq)
    w_x_stage(1, 3)
    w_x_stage(1, 0)
    for kind in range(3):
        f_x_own(kind).start()

    gm_y.wait_send()
    back = gm
    def input_tile(index, carry):
        at = pl.ds(pl.multiple_of(index * span, 128), span)
        back[:, at] = (
            matmul_nt(gq[...], q_w[at, :]) + matmul_nt(gkv[...], kv_w[index].reshape(span, 2 * head))
        ).astype(jnp.bfloat16)
        return carry

    lax.fori_loop(0, z_size, input_tile, 0)
    back_out = remote(back.at[theirs], back_y, y_send.at[1], y_recv.at[1], to_y)
    back_out.start()

    kv_part = kv_w

    def kv_tile(index, carry):
        at = pl.ds(pl.multiple_of(index * span, 128), span)
        product = dot_nn(n1_ref[:, at].T, gkv[...]).astype(jnp.bfloat16)
        kv_part[index] = product.reshape(kv_part.shape[1:])
        return carry

    lax.fori_loop(0, z_size, kv_tile, 0)
    kv_over_y = remote(kv_part.at[:, :, :, 1 - me_y], kv_y, y_send.at[2], y_recv.at[2], to_y)
    kv_over_y.start()
    mix_step(2)
    w_z_stage(0, 2)
    mix_step(3)
    w_z_stage(0, 3)

    back_out.wait_recv()

    def input_rows(index, total):
        at = pl.ds(pl.multiple_of(index * 32, 32), 32)
        there = pl.ds(pl.multiple_of(me_y * own + index * 32, 32), 32)
        upstream = back[there, :].astype(jnp.float32) + back_y[at, :].astype(jnp.float32)
        grad, gain_part = norm_back(
            tok_ref[at, :].astype(jnp.float32), gain_ref[0:1, :], upstream
        )
        tgrad_ref[at, :] = (gm_f[at, :] + grad).astype(jnp.bfloat16)
        return total + gain_part

    attn_gain_part = lax.fori_loop(
        0, own // 32, input_rows, jnp.zeros((1, width), jnp.float32)
    )
    for index in range(4):
        at = slice(index * span, (index + 1) * span)
        gain_own[0, index : index + 1, :] = attn_gain_part[:, at]
        gain_own[0, 4 + index : 5 + index, :] = gain_part_ref[4 + index : 5 + index, :]

    def gain_send(stage, where):
        return remote(
            gain_own.at[stage], gain_in.at[stage], g_send.at[stage], g_recv.at[stage], where
        )

    gain_hops = [gain_send(0, to_y), gain_send(1, to_c), gain_send(2, to_x)]
    gain_last = [
        remote(
            gain_own.at[3], gain_in.at[2 + step], g_send.at[2 + step], g_recv.at[2 + step], to_z(step)
        )
        for step in range(1, z_size)
    ]

    def gain_fold(stage):
        gain_hops[stage].wait_recv()
        gain_own[stage + 1] = gain_own[stage] + gain_in[stage]

    gain_hops[0].start()
    mid_load.start()
    w_z_stage(1, 1)
    w_z_stage(0, 0)
    w_z_stage(1, 2)
    gain_fold(0)
    gain_hops[1].start()
    mix_step(0)
    w_z_stage(1, 3)
    gain_fold(1)
    gain_hops[2].start()
    kv_over_y.wait_recv()

    def kv_add_y(index, carry):
        for x_at in range(2):
            for c_at in range(2):
                block = kv_part.at[index, x_at, c_at, me_y]
                block[...] = (
                    block[...].astype(jnp.float32) + kv_y[index, x_at, c_at].astype(jnp.float32)
                ).astype(jnp.bfloat16)
        return carry

    lax.fori_loop(0, z_size, kv_add_y, 0)
    kv_over_c = remote(
        kv_part.at[:, :, 1 - me_c, me_y], kv_c, kc_send.at[0], kc_recv.at[0], to_c
    )
    kv_over_c.start()
    gain_fold(2)
    for copy in gain_last:
        copy.start()
    kv_over_c.wait_recv()

    def kv_add_c(index, carry):
        for x_at in range(2):
            block = kv_part.at[index, x_at, me_c, me_y]
            block[...] = (
                block[...].astype(jnp.float32) + kv_c[index, x_at].astype(jnp.float32)
            ).astype(jnp.bfloat16)
        return carry

    lax.fori_loop(0, z_size, kv_add_c, 0)
    kv_over_x = remote(
        kv_part.at[:, 1 - me_x, me_c, me_y], kv_x, kc_send.at[1], kc_recv.at[1], to_x
    )
    kv_over_x.start()
    w_z_stage(1, 0)
    kv_over_x.wait_recv()

    def kv_add_x(index, carry):
        block = kv_part.at[index, me_x, me_c, me_y]
        block[...] = (
            block[...].astype(jnp.float32) + kv_x[index].astype(jnp.float32)
        ).astype(jnp.bfloat16)
        return carry

    lax.fori_loop(0, z_size, kv_add_x, 0)
    kv_over_z = [
        remote(
            kv_part.at[lax.rem(me_z + step, z_size), me_x, me_c, me_y],
            kv_z.at[step - 1],
            kz_send.at[step],
            kz_recv.at[step],
            to_z(step),
        )
        for step in range(1, z_size)
    ]
    for copy in kv_over_z:
        copy.start()
    for copy in gain_last:
        copy.wait_recv()
    gsum_ref[...] = gain_own[3] + gain_in[3] + gain_in[4] + gain_in[5]
    for copy in kv_over_z:
        copy.wait_recv()
    kvg_ref[...] = (
        kv_part[me_z, me_x, me_c, me_y].astype(jnp.float32)
        + kv_z[0].astype(jnp.float32)
        + kv_z[1].astype(jnp.float32)
        + kv_z[2].astype(jnp.float32)
    )

    back_out.wait_send()
    kv_over_y.wait_send()
    kv_over_c.wait_send()
    kv_over_x.wait_send()
    for kind in range(3):
        f_x_own(kind).wait()
    for index in range(len(tasks)):
        f_x(index).wait_send()
    for step in range(1, z_size):
        for kind in range(3):
            f_z(step, kind, me_z, lambda copy: copy.wait_send())
            f_z(step, kind, behind(step), lambda copy: copy.wait_recv())
    for copy in gain_hops + gain_last + kv_over_z:
        copy.wait_send()
    for step in range(z_size):
        mix_over_y(step).wait_send()
        if step:
            mix_over_z(step).wait_send()
        for kind in range(2):
            w_c(kind, step, 0).wait_send()
            w_c(kind, step, 1).wait_send()
            w_x(kind, step).wait_send()
            if step:
                w_z(kind, step).wait_send()


def post_call(
    tokens,
    gains,
    gain_part,
    normed_one,
    rotated,
    keys,
    values,
    attn_vals,
    table,
    allowed,
    kv_weight,
    query_weight,
    out_weight,
    mix_parts,
    grad_mid,
    grad_mid_low,
    mid,
    ffn_sums,
    main,
):
    z_size = lax.axis_size("z")
    own, width = tokens.shape
    seq = 2 * own
    head = keys.shape[1]
    cols = attn_vals.shape[1]
    rows = width // (4 * z_size)
    units = ffn_sums.shape[4]
    low = lambda *dims: pltpu.VMEM(dims, jnp.bfloat16)
    full = lambda *dims: pltpu.VMEM(dims, jnp.float32)
    out_full = lambda *dims: jax.ShapeDtypeStruct(dims, jnp.float32)
    out_low = lambda *dims: jax.ShapeDtypeStruct(dims, jnp.bfloat16)
    dma = lambda *lead: pltpu.SemaphoreType.DMA(lead)
    vmem = pl.BlockSpec(memory_space=pltpu.VMEM)
    hbm = pl.BlockSpec(memory_space=pl.ANY)
    z = z_size
    return pl.pallas_call(
        functools.partial(post_kernel, z_size, main),
        out_shape=(
            out_low(own, width),
            out_low(own, width),
            out_full(8, width // z),
            out_full(rows // 2, 2 * head),
            out_full(rows, cols),
            out_full(rows, cols),
            out_low(3, z, rows, units),
        ),
        in_specs=[vmem] * 11 + [hbm] * 8,
        out_specs=(vmem,) * 6 + (hbm,),
        scratch_shapes=[
            low(z, 2, 2, 2, rows // 2, 2 * head),
            low(width, cols),
            low(width, cols),
            low(width, cols),
            low(seq, width),
            full(own, width),
            low(seq, cols),
            low(seq, 2 * head),
            full(2, seq, head),
            low(own, width),
            low(z, width, own),
            low(z + 1, width, own),
            low(z, width, own),
            low(z, 2, rows, cols),
            low(z, rows, cols),
            low(z + 1, rows, cols),
            low(z, 2, rows, cols),
            low(z, rows, cols),
            low(z + 1, rows, cols),
            low(z, 2, 2, rows // 2, 2 * head),
            low(z, 2, rows // 2, 2 * head),
            low(z, rows // 2, 2 * head),
            low(z - 1, rows // 2, 2 * head),
            full(4, 8, width // z),
            full(6, 8, width // z),
            low(6, rows, units),
            low(2, rows, units),
            dma(6 + z),
            dma(2),
            dma(9),
            dma(9),
            dma(3, z),
            dma(3, z),
            dma(3),
            dma(3),
            dma(z),
            dma(z),
            dma(z),
            dma(z + 1),
            dma(2, z, 2),
            dma(2, z, 2),
            dma(2, z),
            dma(2, z),
            dma(2, z),
            dma(2, z + 1),
            dma(2),
            dma(2),
            dma(z),
            dma(z),
            dma(6),
            dma(6),
        ],
        compiler_params=pltpu.CompilerParams(
            collective_id=2, has_side_effects=True, vmem_limit_bytes=VMEM_BYTES
        ),
        cost_estimate=pl.CostEstimate(
            flops=14 * seq * width * cols,
            bytes_accessed=10 * width * cols,
            transcendentals=seq * seq * cols // head,
        ),
    )(
        tokens,
        gains,
        gain_part,
        normed_one,
        rotated,
        keys,
        values,
        attn_vals,
        *table,
        allowed,
        kv_weight.reshape(z, 2, 2, 2, rows // 2, kv_weight.shape[1]),
        query_weight,
        out_weight,
        mix_parts,
        grad_mid,
        grad_mid_low,
        mid,
        ffn_sums,
    )


def layout_kernel(
    z_size,
    main,
    sum_ref,
    ffn_ref,
    q_ref,
    o_ref,
    kv_ref,
    mixed_in,
    tgrad_in,
    wg_ref,
    wu_ref,
    wd_ref,
    qg_ref,
    og_ref,
    kvg_ref,
    mixed_ref,
    tgrad_ref,
):
    me_z = lax.axis_index("z")
    for kind, out in enumerate((wg_ref, wu_ref, wd_ref)):
        for step in range(z_size):
            at = lax.rem(me_z - step + z_size, z_size)
            values = ffn_ref[kind, step].astype(jnp.float32)
            if step == 0:
                values = values + sum_ref[kind, 0, 0].astype(jnp.float32)
            body = pl.ds(pl.multiple_of(at * main, 128), main)
            out[:, body] = values[:, :main]

            @pl.when((at > 0) & (at < z_size - 1))
            def _(out=out, at=at, values=values):
                tail = z_size * main + lax.rem(at + 1, 2) * 128
                out[:, pl.ds(pl.multiple_of(tail, 128), 128)] = values[:, main:]
    qg_ref[...] = q_ref[...]
    og_ref[...] = o_ref[...]
    kvg_ref[...] = kv_ref[...]
    mixed_ref[...] = mixed_in[...]
    tgrad_ref[...] = tgrad_in[...]


def layout_call(ffn_sums, ffn_grads, query_grad, out_grad, kv_grad, mixed, tokens_grad, ffn_cols):
    z_size = lax.axis_size("z")
    main, units = ragged_split(ffn_cols, z_size)
    rows, cols = query_grad.shape
    parts = rows // 80
    kv_rows = kv_grad.shape[0] // parts
    full = lambda *dims: jax.ShapeDtypeStruct(dims, jnp.float32)
    row = lambda height, width: pl.BlockSpec((height, width), lambda index: (index, 0))
    own, width = mixed.shape
    share = pl.BlockSpec((own, width // parts), lambda index: (0, index))
    specs = [row(80, cols), row(80, cols), row(kv_rows, kv_grad.shape[1]), share, share]
    return pl.pallas_call(
        functools.partial(layout_kernel, z_size, main),
        grid=(parts,),
        out_shape=(
            *[full(rows, ffn_cols)] * 3,
            full(rows, cols),
            full(rows, cols),
            full(*kv_grad.shape),
            jax.ShapeDtypeStruct(mixed.shape, jnp.bfloat16),
            jax.ShapeDtypeStruct(mixed.shape, jnp.bfloat16),
        ),
        in_specs=[
            pl.BlockSpec((3, 1, 1, 80, units), lambda index: (0, 0, 0, index, 0)),
            pl.BlockSpec((3, z_size, 80, units), lambda index: (0, 0, index, 0)),
            *specs,
        ],
        out_specs=(*[row(80, ffn_cols)] * 3, *specs),
        compiler_params=pltpu.CompilerParams(vmem_limit_bytes=VMEM_BYTES),
    )(ffn_sums, ffn_grads, query_grad, out_grad, kv_grad, mixed, tokens_grad)


FF_SPLIT = 4


def ffn_pass(normed, grad_out, gate_weight, up_weight, down_weight):
    gate = jnp.dot(normed, gate_weight, preferred_element_type=jnp.float32)
    up_proj = jnp.dot(normed, up_weight, preferred_element_type=jnp.float32)
    grad_hidden = jnp.dot(grad_out, down_weight, preferred_element_type=jnp.float32)
    product, pull = jax.vjp(gelu_product, gate, up_proj)
    hidden = product.astype(jnp.bfloat16)
    grad_gate_f, grad_up_f = pull(grad_hidden)
    grad_gate = grad_gate_f.astype(jnp.bfloat16)
    grad_up = grad_up_f.astype(jnp.bfloat16)
    mixed_part = matmul_nt(hidden, down_weight).astype(jnp.bfloat16)
    normed_part = (matmul_nt(grad_gate, gate_weight) + matmul_nt(grad_up, up_weight)).astype(
        jnp.bfloat16
    )
    weight_parts = [
        matmul_tn(normed, grad_gate).astype(jnp.bfloat16),
        matmul_tn(normed, grad_up).astype(jnp.bfloat16),
        matmul_tn(grad_out, hidden).astype(jnp.bfloat16),
    ]
    return mixed_part, normed_part, weight_parts


def shards_general(
    tokens,
    segments,
    positions,
    cotangent,
    attn_gain,
    ffn_gain,
    w_kv,
    w_query,
    w_out,
    w_gate,
    w_up,
    w_down,
):
    everywhere = ("z", "xc", "mp")
    dp = ("z", "xc")
    z_size = lax.axis_size("z")
    xc_size = lax.axis_size("xc")
    gains = lax.all_gather(
        jnp.stack([attn_gain, ffn_gain], axis=1), everywhere, axis=0, tiled=True
    ).astype(jnp.float32)
    gain_one, gain_two = gains[:, 0], gains[:, 1]
    kv_weight = lax.all_gather(w_kv, everywhere, axis=0, tiled=True)
    head_dim = kv_weight.shape[1] // 2
    width = tokens.shape[1]
    seq_len = segments.shape[0]
    heads_here = w_query.shape[1] // head_dim
    scale = head_dim ** (-0.5)
    cosine, sine = rotary_angles(positions, head_dim)
    inputs_f = tokens.astype(jnp.float32)
    tokens_all = lax.all_gather(tokens, "mp", axis=0, tiled=True)
    normed_one = norm_gain(tokens_all.astype(jnp.float32), gain_one).astype(jnp.bfloat16)
    query_weight = lax.all_gather(w_query, dp, axis=0, tiled=True)
    out_weight = lax.all_gather(w_out, dp, axis=0, tiled=True)

    rows = w_gate.shape[0]
    unit = w_gate.shape[1] // z_size

    def spread(weight):
        pieces = weight.reshape(rows, z_size, unit).transpose(1, 0, 2)
        pieces = lax.all_to_all(pieces, "z", split_axis=0, concat_axis=0, tiled=True)
        return lax.all_gather(pieces, "xc", axis=1, tiled=False).reshape(width, unit)

    gate_weight, up_weight, down_weight = spread(w_gate), spread(w_up), spread(w_down)
    grad_all = lax.all_gather(cotangent, ("z", "mp"), axis=0, tiled=True)

    query = jnp.dot(normed_one, query_weight, preferred_element_type=jnp.float32).reshape(
        seq_len, heads_here, head_dim
    )
    rotated = (rotate(query, cosine[:, None], sine[:, None]) * scale).astype(jnp.bfloat16)
    keyval = jnp.dot(normed_one, kv_weight, preferred_element_type=jnp.float32)
    keys = rotate(keyval[:, :head_dim], cosine, sine).astype(jnp.bfloat16)
    values = keyval[:, head_dim:].astype(jnp.bfloat16)
    allowed = block_allowed(segments, 0, seq_len)
    scores = jnp.einsum("thd,sd->hts", rotated, keys, preferred_element_type=jnp.float32)
    scores = jnp.where(allowed[None], scores, masked_score)
    row_max = jnp.max(scores, axis=-1, keepdims=True)
    weights = jnp.exp(scores - row_max)
    probs = weights / jnp.sum(weights, axis=-1, keepdims=True)
    probs_low = probs.astype(jnp.bfloat16)
    attn_vals = (
        jnp.einsum("hts,sd->thd", probs_low, values, preferred_element_type=jnp.float32)
        .reshape(seq_len, heads_here * head_dim)
        .astype(jnp.bfloat16)
    )
    mid = inputs_f + lax.psum_scatter(
        matmul_nt(attn_vals, out_weight).astype(jnp.bfloat16),
        "mp",
        scatter_dimension=0,
        tiled=True,
    ).astype(jnp.float32)
    normed_two = norm_gain(mid, gain_two).astype(jnp.bfloat16)
    normed_all = lax.all_gather(normed_two, ("z", "mp"), axis=0, tiled=True)

    mixed_part, normed_part, weight_parts = ffn_pass(
        normed_all, grad_all, gate_weight, up_weight, down_weight
    )
    grad_normed_two = lax.psum_scatter(
        normed_part, ("z", "mp"), scatter_dimension=0, tiled=True
    ).astype(jnp.float32)
    mixed = (
        mid
        + lax.psum_scatter(mixed_part, ("z", "mp"), scatter_dimension=0, tiled=True).astype(
            jnp.float32
        )
    ).astype(jnp.bfloat16)

    def collect(part):
        pieces = part.reshape(z_size, xc_size, rows, unit).transpose(1, 0, 2, 3)
        pieces = pieces.reshape(xc_size * z_size * rows, unit)
        pieces = lax.psum_scatter(pieces, "xc", scatter_dimension=0, tiled=True)
        pieces = pieces.reshape(z_size, rows, unit)
        pieces = lax.all_to_all(pieces, "z", split_axis=0, concat_axis=0, tiled=True)
        return pieces.transpose(1, 0, 2).reshape(rows, z_size * unit).astype(jnp.float32)

    w_gate_grad, w_up_grad, w_down_grad = [collect(part) for part in weight_parts]

    norm_pull_two = jax.vjp(norm_gain, mid, gain_two)[1]
    grad_mid_norm, grad_gain_two = norm_pull_two(grad_normed_two)
    grad_mid = cotangent.astype(jnp.float32) + grad_mid_norm
    grad_mid_all = lax.all_gather(grad_mid.astype(jnp.bfloat16), "mp", axis=0, tiled=True)
    grad_vals = (
        jnp.dot(grad_mid_all, out_weight, preferred_element_type=jnp.float32)
        .astype(jnp.bfloat16)
        .reshape(seq_len, heads_here, head_dim)
    )
    grad_probs = jnp.einsum("thd,sd->hts", grad_vals, values, preferred_element_type=jnp.float32)
    delta = jnp.sum(probs * grad_probs, axis=-1, keepdims=True)
    grad_scores = (probs * (grad_probs - delta)).astype(jnp.bfloat16)
    grad_rot = jnp.einsum("hts,sd->thd", grad_scores, keys, preferred_element_type=jnp.float32)
    key_sum = jnp.einsum("hts,thd->sd", grad_scores, rotated, preferred_element_type=jnp.float32)
    value_sum = jnp.einsum("hts,thd->sd", probs_low, grad_vals, preferred_element_type=jnp.float32)
    grad_query = (
        (unrotate(grad_rot, cosine[:, None], sine[:, None]) * scale)
        .reshape(seq_len, heads_here * head_dim)
        .astype(jnp.bfloat16)
    )
    grad_kv = jnp.concatenate([unrotate(key_sum, cosine, sine), value_sum], axis=1).astype(
        jnp.bfloat16
    )
    grad_normed_one = lax.psum_scatter(
        (matmul_nt(grad_query, query_weight) + matmul_nt(grad_kv, kv_weight)).astype(jnp.bfloat16),
        "mp",
        scatter_dimension=0,
        tiled=True,
    ).astype(jnp.float32)
    norm_pull_one = jax.vjp(norm_gain, inputs_f, gain_one)[1]
    grad_input_norm, grad_gain_one = norm_pull_one(grad_normed_one)
    tokens_grad = (grad_mid + grad_input_norm).astype(jnp.bfloat16)

    w_query_grad = lax.psum_scatter(
        matmul_tn(normed_one, grad_query).astype(jnp.bfloat16), dp, scatter_dimension=0, tiled=True
    ).astype(jnp.float32)
    w_out_grad = lax.psum_scatter(
        matmul_tn(grad_mid_all, attn_vals).astype(jnp.bfloat16), dp, scatter_dimension=0, tiled=True
    ).astype(jnp.float32)
    small = jnp.concatenate(
        [matmul_tn(normed_one, grad_kv), grad_gain_one[:, None], grad_gain_two[:, None]], axis=1
    )
    small = lax.psum_scatter(small, everywhere, scatter_dimension=0, tiled=True)
    kv_grad = small[:, : 2 * head_dim]
    return (
        mixed,
        tokens_grad,
        small[:, 2 * head_dim],
        small[:, 2 * head_dim + 1],
        kv_grad,
        w_query_grad,
        w_out_grad,
        w_gate_grad,
        w_up_grad,
        w_down_grad,
    )


def shards_fast(
    tokens,
    segments,
    positions,
    cotangent,
    attn_gain,
    ffn_gain,
    w_kv,
    w_query,
    w_out,
    w_gate,
    w_up,
    w_down,
):
    quarter = w_kv.shape[1] // 8
    lane = jnp.arange(2 * quarter)
    freqs = rope_base ** (-(lane % quarter).astype(jnp.float32) / quarter)
    phase = positions.astype(jnp.float32)[:, None] * freqs[None, :]
    table = (jnp.cos(phase), jnp.where(lane < quarter, -1.0, 1.0)[None, :] * jnp.sin(phase))
    (
        normed_one,
        rotated,
        keys,
        values,
        attn_vals,
        mid,
        normed_two,
        gains,
        allowed,
        kv_weight,
        query_weight,
        out_weight,
        ffn_weights,
        grad_all,
    ) = pre_call(
        tokens,
        w_kv,
        attn_gain[None, :],
        ffn_gain[None, :],
        table,
        segments[None, :],
        cotangent,
        w_query,
        w_out,
        (w_gate, w_up, w_down),
    )
    main = ragged_split(w_gate.shape[1], lax.axis_size("z"))[0]
    grad_mid, gain_part, mix_parts, ffn_sums, grad_mid_low = ffn_call(
        gains, normed_two, grad_all, ffn_weights, mid, w_gate.shape[0], main
    )
    mixed, tokens_grad, gain_grads, kv_grad, query_grad, out_grad, ffn_grads = post_call(
        tokens,
        gains,
        gain_part,
        normed_one,
        rotated,
        keys,
        values,
        attn_vals,
        table,
        allowed,
        kv_weight,
        query_weight,
        out_weight,
        mix_parts,
        grad_mid,
        grad_mid_low,
        mid,
        ffn_sums,
        main,
    )
    *ffn_out, query_grad, out_grad, kv_grad, mixed, tokens_grad = layout_call(
        ffn_sums,
        ffn_grads,
        query_grad,
        out_grad,
        kv_grad,
        mixed,
        tokens_grad,
        w_gate.shape[1],
    )
    share = attn_gain.shape[0]
    place = lax.axis_index(("z", "x", "c", "mp")) * share
    gain_grads = gain_grads.reshape(2, gain_grads.size // 2)
    gain_grads = lax.dynamic_slice(gain_grads, (0, place), (2, share))
    return (
        mixed,
        tokens_grad,
        gain_grads[0],
        gain_grads[1],
        kv_grad,
        query_grad,
        out_grad,
        *ffn_out,
    )


def solution(mesh):
    dp_size, mp_size = mesh.shape["dp"], mesh.shape["mp"]
    if dp_size == 4 * FF_SPLIT and mp_size == 2:
        body, dp = shards_fast, ("z", "x", "c")
        sizes = (FF_SPLIT, 2, 2, mp_size)
    else:
        body, dp = shards_general, ("z", "xc")
        sizes = (FF_SPLIT, dp_size // FF_SPLIT, mp_size)
    all_axes = (*dp, "mp")
    fine = jax.sharding.Mesh(mesh.devices.reshape(sizes), all_axes)
    in_specs = (
        P(all_axes, None),
        P(dp),
        P(dp),
        P(all_axes, None),
        P(all_axes),
        P(all_axes),
        P(all_axes, None),
        P(dp, "mp"),
        P(dp, "mp"),
        P(dp, "mp"),
        P(dp, "mp"),
        P(dp, "mp"),
    )
    out_specs = (
        P(all_axes, None),
        P(all_axes, None),
        P(all_axes),
        P(all_axes),
        P(all_axes, None),
        P(dp, "mp"),
        P(dp, "mp"),
        P(dp, "mp"),
        P(dp, "mp"),
        P(dp, "mp"),
    )
    return jax.shard_map(body, mesh=fine, in_specs=in_specs, out_specs=out_specs, check_vma=False)
```

```python
import functools

import jax
import jax.numpy as jnp
from jax import lax
from jax.experimental import pallas as pl
from jax.experimental.pallas import tpu as pltpu
from jax.sharding import PartitionSpec as P

WINDOW = 2048


epsilon = 1e-06
rope_base = 10000.0
masked_score = -1e30
VMEM_BYTES = 66_000_000


def norm_gain(values, gain):
    return values * lax.rsqrt(jnp.mean(values * values, axis=-1, keepdims=True) + epsilon) * gain


def rotary_angles(positions, head_width):
    quarter = head_width // 4
    freqs = rope_base ** (-jnp.arange(quarter).astype(jnp.float32) / quarter)
    phase = positions.astype(jnp.float32)[:, None] * freqs[None, :]
    return (jnp.cos(phase), jnp.sin(phase))


def rotate(values, cosine, sine):
    quarter = cosine.shape[-1]
    first_half = values[..., :quarter]
    second_half = values[..., quarter : 2 * quarter]
    return jnp.concatenate(
        [
            first_half * cosine - second_half * sine,
            second_half * cosine + first_half * sine,
            values[..., 2 * quarter :],
        ],
        axis=-1,
    )


def unrotate(values, cosine, sine):
    quarter = cosine.shape[-1]
    first_half = values[..., :quarter]
    second_half = values[..., quarter : 2 * quarter]
    return jnp.concatenate(
        [
            first_half * cosine + second_half * sine,
            second_half * cosine - first_half * sine,
            values[..., 2 * quarter :],
        ],
        axis=-1,
    )


def gelu_product(gate, up_proj):
    return jax.nn.gelu(gate, approximate=True) * up_proj


def matmul_nt(left, right):
    return lax.dot_general(
        left, right, (((1,), (1,)), ((), ())), preferred_element_type=jnp.float32
    )


def matmul_tn(left, right):
    return lax.dot_general(
        left, right, (((0,), (0,)), ((), ())), preferred_element_type=jnp.float32
    )


def block_allowed(segments, first_row, rows):
    seq_len = segments.shape[0]
    query_rows = first_row + jnp.arange(rows)
    key_rows = jnp.arange(seq_len)
    return (
        (segments[:, None] == segments[None, :])
        & (key_rows[None, :] <= query_rows[:, None])
        & (query_rows[:, None] - key_rows[None, :] < WINDOW)
    )


MESH_ID = pl.DeviceIdType.MESH
GELU_A = 0.7978845608028654
GELU_B = 0.044715
TILE = 256
WIDE = 512


def remote(src, dst, send_sem, recv_sem, where):
    return pltpu.make_async_remote_copy(
        src_ref=src,
        dst_ref=dst,
        send_sem=send_sem,
        recv_sem=recv_sem,
        device_id=where,
        device_id_type=MESH_ID,
    )


class Halves:
    def __init__(self, src, dst, send_sem, recv_sem, where):
        rows = src.shape[0] // 2
        cuts = [pl.ds(part * rows, rows) for part in range(2)]
        self.copies = [
            remote(src.at[cut], dst.at[cut], send_sem.at[part], recv_sem.at[part], where)
            for part, cut in enumerate(cuts)
        ]

    def start(self):
        for copy in self.copies:
            copy.start()

    def wait_recv(self):
        for copy in self.copies:
            copy.wait_recv()

    def wait_send(self):
        for copy in self.copies:
            copy.wait_send()


def dot_nn(left, right):
    return lax.dot_general(
        left, right, (((1,), (0,)), ((), ())), preferred_element_type=jnp.float32
    )


def gelu_parts(gate):
    square = gate * gate
    bend = jnp.tanh(GELU_A * gate * (1.0 + GELU_B * square))
    half = 0.5 * (1.0 + bend)
    slope = half + 0.5 * gate * (1.0 - bend * bend) * GELU_A * (1.0 + 3.0 * GELU_B * square)
    return gate * half, slope


def add_rows(first, rest, out, count):
    def body(index, carry):
        step = pl.ds(pl.multiple_of(index * 32, 32), 32)
        total = first[step, :].astype(jnp.float32)
        for other in rest:
            total = total + other[step, :].astype(jnp.float32)
        out[step, :] = total.astype(out.dtype)
        return carry

    lax.fori_loop(0, count // 32, body, 0)


def norm_back(values, gain, upstream):
    scale = lax.rsqrt(jnp.mean(values * values, axis=-1, keepdims=True) + epsilon)
    normed = values * scale
    pulled = gain * upstream
    back = scale * (pulled - normed * jnp.mean(normed * pulled, axis=-1, keepdims=True))
    return back, jnp.sum(upstream * normed, axis=0, keepdims=True)


def ffn_kernel(
    z_size,
    main,
    gain_ref,
    own_hbm,
    dy_hbm,
    w_hbm,
    mid_hbm,
    gm_ref,
    gain_part,
    mix_hbm,
    sums_hbm,
    gm_hbm,
    n2,
    dy,
    w3,
    h3,
    n2_t,
    dy_t,
    gn_part,
    mix_buf,
    gn_y,
    gn_z,
    gn_s,
    c_in,
    x_in,
    mid,
    load_sem,
    mix_sem,
    ag_y_send,
    ag_y_recv,
    ag_z_send,
    ag_z_recv,
    rs_y_send,
    rs_y_recv,
    rs_z_send,
    rs_z_recv,
    c_send,
    c_recv,
    x_send,
    x_recv,
    out_sem,
):
    own = own_hbm.shape[0] // 2
    width = own_hbm.shape[1]
    units = w3.shape[2]
    rows = c_in.shape[3]
    span = width // z_size
    me_y, me_z = lax.axis_index("mp"), lax.axis_index("z")
    me_x, me_c = lax.axis_index("x"), lax.axis_index("c")
    mine = pl.ds(pl.multiple_of(me_y * own, own), own)
    theirs = pl.ds(pl.multiple_of((1 - me_y) * own, own), own)
    to_y, to_x, to_c = {"mp": 1 - me_y}, {"x": 1 - me_x}, {"c": 1 - me_c}

    def ahead(step):
        return lax.rem(me_z + step, z_size)

    def to_z(step):
        return {"z": ahead(step)}

    def row_block(z_at, x_at, c_at):
        return pl.ds(pl.multiple_of(((z_at * 2 + x_at) * 2 + c_at) * rows, rows), rows)

    inner = (me_z > 0) & (me_z < z_size - 1)
    outer = (me_z == 0) | (me_z == z_size - 1)

    def w_load(index, columns):
        cols = pl.ds(0, columns)
        return pltpu.make_async_copy(
            w_hbm.at[index, :, cols], w3.at[index, :, cols], load_sem.at[z_size + index]
        )

    def w_loads(act):
        for case, columns in ((inner, units), (outer, main)):

            @pl.when(case)
            def _(columns=columns):
                for index in range(3):
                    act(w_load(index, columns))

    w_loads(lambda copy: copy.start())
    dy_loads = [
        pltpu.make_async_copy(dy_hbm.at[index], dy, load_sem.at[index])
        for index in range(z_size)
    ]
    own_load = pltpu.make_async_copy(own_hbm, n2.at[0], load_sem.at[z_size + 3])
    mid_load = pltpu.make_async_copy(mid_hbm, mid, load_sem.at[z_size + 4])
    for load in (own_load, dy_loads[0], mid_load):
        load.start()

    barrier = pltpu.get_barrier_semaphore()
    peers = [to_y, to_x, to_c] + [to_z(step) for step in range(1, z_size)]
    for where in peers:
        pl.semaphore_signal(barrier, inc=1, device_id=where, device_id_type=MESH_ID)
    pl.semaphore_wait(barrier, len(peers))

    def ag_y(index):
        block = n2.at[index, mine]
        return Halves(block, block, ag_y_send.at[index], ag_y_recv.at[index], to_y)

    def ag_y_in(index):
        block = n2.at[index, theirs]
        return Halves(block, block, ag_y_send.at[index], ag_y_recv.at[index], to_y)

    def ag_z(index):
        src = own_hbm.at[mine] if index == 0 else n2.at[index, mine]
        return Halves(
            src, n2.at[index + 1, mine], ag_z_send.at[index], ag_z_recv.at[index + 1], to_z(1)
        )

    def ag_z_in(index):
        block = n2.at[index, mine]
        return Halves(block, block, ag_z_send.at[0], ag_z_recv.at[index], to_z(1))

    def ag_last():
        return Halves(
            n2.at[2, theirs], n2.at[3, theirs], ag_y_send.at[3], ag_y_recv.at[3], to_z(1)
        )

    def forward(index):
        ag_z_in(index).wait_recv()
        ag_z(index).start()
        ag_y(index).start()

    ag_z(0).start()

    mix_copies = []

    def turn(source, target, index):
        def turn_tile(tile, carry):
            at = pl.ds(pl.multiple_of(tile * span, 128), span)
            target[at, pl.ds(index * 2 * own, 2 * own)] = source[:, at].T
            return carry

        lax.fori_loop(0, z_size, turn_tile, 0)

    def chunk(index):
        if index:
            mix_copies[index - 1].wait()
        dy_loads[index].wait()
        rows_at = pl.ds(index * 2 * own, 2 * own)

        def up_tile(tile, carry):
            cols = pl.ds(pl.multiple_of(tile * WIDE, WIDE), WIDE)
            gate = dot_nn(n2[index], w3[0, :, cols])
            up_proj = dot_nn(n2[index], w3[1, :, cols])
            grad_hidden = dot_nn(dy[...], w3[2, :, cols])
            act, slope = gelu_parts(gate)
            h3[0, rows_at, cols] = (grad_hidden * up_proj * slope).astype(jnp.bfloat16)
            h3[1, rows_at, cols] = (grad_hidden * act).astype(jnp.bfloat16)
            h3[2, rows_at, cols] = (act * up_proj).astype(jnp.bfloat16)
            return carry

        lax.fori_loop(0, units // WIDE, up_tile, 0)

        def down_tile(tile, carry):
            at = pl.ds(pl.multiple_of(tile * span, 128), span)
            normed = matmul_nt(w3[0, at, :], h3[0, rows_at, :]) + matmul_nt(
                w3[1, at, :], h3[1, rows_at, :]
            )
            mixed = matmul_nt(w3[2, at, :], h3[2, rows_at, :])
            for half in range(2):
                cols = slice(half * own, (half + 1) * own)
                gn_part[index, half, at, :] = normed[:, cols].astype(jnp.bfloat16)
                mix_buf[half, at, :] = mixed[:, cols].astype(jnp.bfloat16)
            return carry

        lax.fori_loop(0, z_size, down_tile, 0)
        copy = pltpu.make_async_copy(mix_buf, mix_hbm.at[index], mix_sem.at[index])
        copy.start()
        mix_copies.append(copy)
        if index:
            rs_y(index).start()
        turn(n2.at[index], n2_t, index)
        turn(dy, dy_t, index)
        if index + 1 < z_size:
            dy_loads[index + 1].start()

    def rs_y(index):
        return Halves(
            gn_part.at[index, 1 - me_y], gn_y.at[index], rs_y_send.at[index], rs_y_recv.at[index], to_y
        )

    def rs_z(index):
        return Halves(
            gn_s.at[index - 1],
            gn_z.at[index - 1],
            rs_z_send.at[index],
            rs_z_recv.at[index - 1],
            to_z(1),
        )

    def rs_step(index):
        rs_y(index).wait_recv()
        slot = (index - 2) % z_size
        if index != 1:
            Halves(
                gn_s.at[slot], gn_z.at[slot], rs_z_send.at[1], rs_z_recv.at[slot], to_z(1)
            ).wait_recv()

        def add_tile(tile, carry):
            at = pl.ds(pl.multiple_of(tile * TILE, TILE), TILE)
            total = gn_part[index, me_y, at, :].astype(jnp.float32) + gn_y[index, at, :].astype(
                jnp.float32
            )
            if index != 1:
                total = total + gn_z[slot, at, :].astype(jnp.float32)
            if index == 0:
                gm_ref[:, at] = total.T
            else:
                gn_s[index - 1, at, :] = total.astype(jnp.bfloat16)
            return carry

        lax.fori_loop(0, width // TILE, add_tile, 0)
        if index != 0:
            rs_z(index).start()


    def grads(step):
        at = pl.ds(pl.multiple_of(ahead(step) * span, 128), span)
        for kind, source in enumerate((n2_t, n2_t, dy_t)):

            def tile_body(tile, carry, kind=kind, source=source):
                cols = pl.ds(pl.multiple_of(tile * WIDE, WIDE), WIDE)
                w3[kind, at, cols] = dot_nn(source[at, :], h3[kind, :, cols]).astype(jnp.bfloat16)
                return carry

            lax.fori_loop(0, units // WIDE, tile_body, 0)
            for far in (1, 0):
                over_c(kind, step, far).start()

    def over_c(kind, step, far):
        x_at = 1 - me_x if far else me_x
        return remote(
            w3.at[kind, row_block(ahead(step), x_at, 1 - me_c)],
            c_in.at[kind, step, far],
            c_send.at[kind, step, far],
            c_recv.at[kind, step, far],
            to_c,
        )

    def over_x(kind):
        return remote(
            w3.at[kind, row_block(ahead(1), 1 - me_x, me_c)],
            x_in.at[kind],
            x_send.at[kind],
            x_recv.at[kind],
            to_x,
        )

    out_copies = []

    def keep(kind, step, far, block):
        copy = pltpu.make_async_copy(
            block, sums_hbm.at[kind, step, far], out_sem.at[kind, step, far]
        )
        copy.start()
        out_copies.append(copy)

    def core_sums(step):
        pairs = [(kind, far) for kind in range(3) for far in (1, 0)]
        if step == 1:
            pairs.sort(key=lambda pair: -pair[1])
        for kind, far in pairs:
            over_c(kind, step, far).wait_recv()
            x_at = 1 - me_x if far else me_x
            block = w3.at[kind, row_block(ahead(step), x_at, me_c)]
            add_rows(block, [c_in.at[kind, step, far]], block, rows)
            if step != 1:
                keep(kind, step, far, block)
            elif far:
                over_x(kind).start()

    def first_sums():
        for kind in range(3):
            over_x(kind).wait_recv()
            block = w3.at[kind, row_block(ahead(1), me_x, me_c)]
            add_rows(block, [x_in.at[kind]], block, rows)
            keep(kind, 1, 0, block)

    own_load.wait()
    w_loads(lambda copy: copy.wait())

    @pl.when(outer)
    def _():
        w3[:, :, main:] = jnp.zeros((3, width, units - main), jnp.bfloat16)

    chunk(0)
    forward(1)
    forward(2)
    ag_y_in(1).wait_recv()
    chunk(1)
    ag_y_in(2).wait_recv()
    ag_last().start()
    chunk(2)
    rs_step(1)
    ag_z_in(3).wait_recv()
    ag_last().wait_recv()
    chunk(3)
    rs_y(0).start()
    rs_step(2)
    grads(1)
    grads(2)
    core_sums(1)
    rs_step(3)
    grads(3)
    core_sums(2)
    grads(0)
    core_sums(3)
    rs_step(0)
    core_sums(0)

    cot_load = pltpu.make_async_copy(
        dy_hbm.at[0, mine], dy.at[pl.ds(0, own)], load_sem.at[z_size + 3]
    )
    cot_load.start()
    cot_load.wait()
    mid_load.wait()

    def mid_rows(index, total):
        at = pl.ds(pl.multiple_of(index * 32, 32), 32)
        grad, gain_sum = norm_back(mid[at, :], gain_ref[1:2, :], gm_ref[at, :])
        grad = grad + dy[at, :].astype(jnp.float32)
        gm_ref[at, :] = grad
        dy[pl.ds(pl.multiple_of(own + index * 32, 32), 32), :] = grad.astype(jnp.bfloat16)
        return total + gain_sum

    gain_sum = lax.fori_loop(0, own // 32, mid_rows, jnp.zeros((1, width), jnp.float32))
    gm_save = pltpu.make_async_copy(dy.at[pl.ds(own, own)], gm_hbm, load_sem.at[z_size + 3])
    gm_save.start()
    for index in range(4):
        gain_part[index : index + 1, :] = jnp.zeros((1, span), jnp.float32)
        gain_part[4 + index : 5 + index, :] = gain_sum[:, index * span : (index + 1) * span]
    first_sums()
    gm_save.wait()

    for copy in mix_copies[3:] + out_copies:
        copy.wait()
    for index in range(z_size):
        if index in (1, 2):
            ag_y(index).wait_send()
        if index == 3:
            ag_last().wait_send()
        rs_y(index).wait_send()
        if index < z_size - 1:
            ag_z(index).wait_send()
        if index:
            rs_z(index).wait_send()
        for kind in range(3):
            over_c(kind, index, 0).wait_send()
            over_c(kind, index, 1).wait_send()
            if index == 1:
                over_x(kind).wait_send()


def ffn_call(gains, normed, grad_all, weights, mid, rows, main):
    z_size = lax.axis_size("z")
    pair, width = normed.shape
    units = weights.shape[2]
    own = pair // 2
    wide = lambda *lead: pltpu.VMEM((*lead, width), jnp.bfloat16)
    tall = lambda *lead: pltpu.VMEM((*lead, width, own), jnp.bfloat16)
    dma = lambda *lead: pltpu.SemaphoreType.DMA(lead)
    vmem = pl.BlockSpec(memory_space=pltpu.VMEM)
    hbm = pl.BlockSpec(memory_space=pl.ANY)
    return pl.pallas_call(
        functools.partial(ffn_kernel, z_size, main),
        out_shape=(
            jax.ShapeDtypeStruct((own, width), jnp.float32),
            jax.ShapeDtypeStruct((8, width // z_size), jnp.float32),
            jax.ShapeDtypeStruct((z_size, 2, width, own), jnp.bfloat16),
            jax.ShapeDtypeStruct((3, z_size, 2, rows, units), jnp.bfloat16),
            jax.ShapeDtypeStruct((own, width), jnp.bfloat16),
        ),
        in_specs=[vmem, hbm, hbm, hbm, hbm],
        out_specs=(vmem, vmem, hbm, hbm, hbm),
        scratch_shapes=[
            wide(z_size, pair),
            wide(pair),
            pltpu.VMEM(weights.shape, jnp.bfloat16),
            pltpu.VMEM((3, z_size * pair, units), jnp.bfloat16),
            pltpu.VMEM((width, z_size * pair), jnp.bfloat16),
            pltpu.VMEM((width, z_size * pair), jnp.bfloat16),
            tall(z_size, 2),
            tall(2),
            tall(z_size),
            tall(z_size - 1),
            tall(z_size - 1),
            pltpu.VMEM((3, z_size, 2, rows, units), jnp.bfloat16),
            pltpu.VMEM((3, rows, units), jnp.bfloat16),
            pltpu.VMEM((own, width), jnp.float32),
            dma(z_size + 5),
            dma(z_size),
            dma(z_size, 2),
            dma(z_size, 2),
            dma(z_size, 2),
            dma(z_size, 2),
            dma(z_size, 2),
            dma(z_size, 2),
            dma(z_size, 2),
            dma(z_size, 2),
            dma(3, z_size, 2),
            dma(3, z_size, 2),
            dma(3),
            dma(3),
            dma(3, z_size, 2),
        ],
        compiler_params=pltpu.CompilerParams(
            collective_id=0, has_side_effects=True, vmem_limit_bytes=VMEM_BYTES
        ),
        cost_estimate=pl.CostEstimate(
            flops=18 * z_size * pair * width * units,
            bytes_accessed=4 * weights.size + 12 * z_size * pair * width,
            transcendentals=z_size * pair * units,
        ),
    )(gains, normed, grad_all, weights, mid)


def spin(values, table):
    first = values[:, : values.shape[1] // 2]
    turned = first * table[0] + pltpu.roll(first, first.shape[1] // 2, 1) * table[1]
    return jnp.concatenate([turned, values[:, values.shape[1] // 2 :]], axis=1)


def spin_back(values, table):
    first = values[:, : values.shape[1] // 2]
    turned = first * table[0] - pltpu.roll(first, first.shape[1] // 2, 1) * table[1]
    return jnp.concatenate([turned, values[:, values.shape[1] // 2 :]], axis=1)


def head_probs(rotated, keys, allowed):
    scores = jnp.where(allowed > 0.5, matmul_nt(rotated, keys), masked_score)
    weights = jnp.exp(scores - jnp.max(scores, axis=-1, keepdims=True))
    return weights / jnp.sum(weights, axis=-1, keepdims=True)


def ragged_split(columns, parts):
    main = columns // parts // 128 * 128
    return main, main + 128


def pre_kernel(
    z_size,
    tok_ref,
    wkv_ref,
    gain_one_ref,
    gain_two_ref,
    cos_ref,
    sin_ref,
    seg_ref,
    cot_hbm,
    wq_hbm,
    wo_hbm,
    wg_hbm,
    wu_hbm,
    wd_hbm,
    n1_ref,
    rot_ref,
    key_ref,
    val_ref,
    att_ref,
    mid_ref,
    n2_ref,
    gain_ref,
    allow_ref,
    kv_out,
    wq_out,
    wo_out,
    w3_out,
    dy_out,
    kv_w,
    q_w,
    o_w,
    tok,
    part,
    part_y,
    query,
    gain_rows,
    y_send,
    y_recv,
    ky_send,
    ky_recv,
    az_send,
    az_recv,
    ax_send,
    ax_recv,
    ac_send,
    ac_recv,
    fz_send,
    fz_recv,
    fx_send,
    fx_recv,
    fc_send,
    fc_recv,
    dz_send,
    dz_recv,
    dy_send,
    dy_recv,
    local_sem,
):
    me_z, me_x = lax.axis_index("z"), lax.axis_index("x")
    me_c, me_y = lax.axis_index("c"), lax.axis_index("mp")
    own, width = tok_ref.shape
    rows = wq_hbm.shape[0]
    half_rows = wkv_ref.shape[0]
    head = key_ref.shape[1]
    main, units = ragged_split(wg_hbm.shape[1], z_size)
    to_y, to_x, to_c = {"mp": 1 - me_y}, {"x": 1 - me_x}, {"c": 1 - me_c}

    def to_z(step):
        return {"z": lax.rem(me_z + step, z_size)}

    def from_z(step):
        return lax.rem(me_z - step + z_size, z_size)

    def row_block(step, x_at, c_at):
        start = ((from_z(step) * 2 + x_at) * 2 + c_at) * rows
        return pl.ds(pl.multiple_of(start, rows), rows)

    mine = pl.ds(pl.multiple_of(me_y * own, own), own)
    theirs = pl.ds(pl.multiple_of((1 - me_y) * own, own), own)
    bufs = (kv_w, q_w, o_w)
    inputs = (None, wq_hbm, wo_hbm)

    locals_ = []

    def local(src, dst):
        copy = pltpu.make_async_copy(src, dst, local_sem.at[len(locals_)])
        copy.start()
        locals_.append(copy)
        return copy

    here = row_block(0, me_x, me_c)
    own_q = local(wq_hbm, q_w.at[here])
    own_o = local(wo_hbm, o_w.at[here])
    ffn_in = (wg_hbm, wu_hbm, wd_hbm)

    def body_of(target):
        return pl.ds(pl.multiple_of(target * main, 128), main), pl.ds(0, main)

    def tail_of(target):
        start = z_size * main + lax.rem(target + 1, 2) * 128
        return pl.ds(pl.multiple_of(start, 128), 128), pl.ds(main, 128)

    def is_inner(at):
        return (at > 0) & (at < z_size - 1)

    own_f = []
    for kind in range(3):
        src, dst = body_of(me_z)
        own_f.append(local(ffn_in[kind].at[:, src], w3_out.at[kind, here, dst]))

    def own_tail(kind):
        src, dst = tail_of(me_z)
        return pltpu.make_async_copy(
            ffn_in[kind].at[:, src], w3_out.at[kind, here, dst], local_sem.at[12 + kind]
        )

    @pl.when(is_inner(me_z))
    def _():
        for kind in range(3):
            own_tail(kind).start()
    own_d = local(cot_hbm, dy_out.at[0, mine])

    kv_own = pl.ds(pl.multiple_of(here.start + me_y * half_rows, half_rows), half_rows)
    gain_rows[...] = jnp.zeros(gain_rows.shape, jnp.float32)
    gain_rows[0:1, :half_rows] = gain_one_ref[...].astype(jnp.float32)
    gain_rows[1:2, :half_rows] = gain_two_ref[...].astype(jnp.float32)
    spread = gain_rows[...].T
    kv_w[kv_own, : 2 * head] = wkv_ref[...]
    kv_w[kv_own, 2 * head :] = spread[:half_rows, :].astype(jnp.bfloat16)

    barrier = pltpu.get_barrier_semaphore()
    peers = [to_y, to_x, to_c] + [to_z(step) for step in range(1, z_size)]
    for where in peers:
        pl.semaphore_signal(barrier, inc=1, device_id=where, device_id_type=MESH_ID)
    pl.semaphore_wait(barrier, len(peers))

    tok_y = remote(tok_ref, tok.at[mine], y_send.at[1], y_recv.at[1], to_y)
    tok_y_in = remote(tok_ref, tok.at[theirs], y_send.at[1], y_recv.at[1], to_y)
    part_out = remote(part.at[theirs], part_y, y_send.at[2], y_recv.at[2], to_y)
    n2_y = remote(n2_ref.at[mine], n2_ref.at[mine], y_send.at[3], y_recv.at[3], to_y)
    n2_y_in = remote(n2_ref.at[theirs], n2_ref.at[theirs], y_send.at[3], y_recv.at[3], to_y)

    def block_of(kind, step, x_at):
        if kind:
            return row_block(step, x_at, me_c)
        return kv_rows(step, x_at, me_y)

    def kv_rows(step, x_at, y_at):
        start = row_block(step, x_at, me_c).start + y_at * half_rows
        return pl.ds(pl.multiple_of(start, half_rows), half_rows)

    def kv_y(step, far):
        x_at = 1 - me_x if far else me_x
        block = kv_w.at[kv_rows(step, x_at, me_y)]
        slot = step + z_size * far
        return remote(block, block, ky_send.at[slot], ky_recv.at[slot], to_y)

    def kv_y_in(step, far):
        x_at = 1 - me_x if far else me_x
        block = kv_w.at[kv_rows(step, x_at, 1 - me_y)]
        slot = step + z_size * far
        return remote(block, block, ky_send.at[slot], ky_recv.at[slot], to_y)

    def source(kind, step):
        if isinstance(step, int) and step == 0 and kind:
            return inputs[kind]
        return bufs[kind].at[block_of(kind, step, me_x)]

    first_z, last_z = (z_size - 1 - me_z) // (z_size - 1), me_z // (z_size - 1)
    inner = first_z + last_z == 0
    order = (0, 1 + 2 * first_z, 3 - first_z - last_z, 2 - first_z + last_z)
    hops = (
        None,
        (lax.rem(me_z + 1, z_size), 2),
        (lax.rem(me_z + z_size - 1, z_size), 2),
        (lax.rem(3 * (me_z + 3), z_size), lax.rem(2 * me_z + 3, z_size)),
    )

    def a_z_own(kind, right):
        return remote(
            source(kind, 0),
            bufs[kind].at[block_of(kind, 0, me_x)],
            az_send.at[kind, right],
            az_recv.at[kind, 1 if right else z_size - 1],
            to_z(1 if right else z_size - 1),
        )

    def a_z_start(kind):
        @pl.when(last_z == 0)
        def _():
            a_z_own(kind, 1).start()

        @pl.when(first_z == 0)
        def _():
            a_z_own(kind, 0).start()

    def a_z(kind, index):
        target, slot = hops[index]
        block = bufs[kind].at[block_of(kind, order[index], me_x)]
        return remote(
            block, block, az_send.at[kind, 1 + index], az_recv.at[kind, slot], {"z": target}
        )

    def a_z_next(kind, index):
        @pl.when(inner)
        def _():
            a_z(kind, index).start()

    def a_z_done(kind):
        @pl.when(last_z == 0)
        def _():
            a_z_own(kind, 1).wait_send()

        @pl.when(first_z == 0)
        def _():
            a_z_own(kind, 0).wait_send()

        @pl.when(inner)
        def _():
            for index in range(1, z_size):
                a_z(kind, index).wait_send()

    def a_z_in(kind, step):
        block = bufs[kind].at[block_of(kind, step, me_x)]
        return remote(block, block, az_send.at[kind, 0], az_recv.at[kind, step], to_z(1))

    def a_x(kind, step):
        return remote(
            source(kind, step),
            bufs[kind].at[block_of(kind, step, me_x)],
            ax_send.at[kind, step],
            ax_recv.at[kind, step],
            to_x,
        )

    def a_x_in(kind, step):
        block = bufs[kind].at[block_of(kind, step, 1 - me_x)]
        return remote(block, block, ax_send.at[kind, step], ax_recv.at[kind, step], to_x)

    def a_c(kind, step, far):
        x_at = 1 - me_x if far else me_x
        block = bufs[kind].at[row_block(step, x_at, me_c)]
        src = source(kind, step) if kind and not far else block
        slot = step + z_size * far
        return remote(src, block, ac_send.at[kind, slot], ac_recv.at[kind, slot], to_c)

    def a_c_in(kind, step, far):
        x_at = 1 - me_x if far else me_x
        block = bufs[kind].at[row_block(step, x_at, 1 - me_c)]
        slot = step + z_size * far
        return remote(block, block, ac_send.at[kind, slot], ac_recv.at[kind, slot], to_c)

    def f_z(kind, step, act):
        target = lax.rem(me_z + step, z_size)

        def piece(index, src, dst):
            return remote(
                ffn_in[kind].at[:, src],
                w3_out.at[kind, here, dst],
                fz_send.at[kind, step, index],
                fz_recv.at[kind, step, index],
                to_z(step),
            )

        act(piece(0, *body_of(target)))

        @pl.when(is_inner(target))
        def _():
            act(piece(1, *tail_of(target)))

    def f_z_wait(kind, step):
        block = row_block(step, me_x, me_c)

        def piece(index, dst):
            part = w3_out.at[kind, block, dst]
            return remote(
                part, part, fz_send.at[kind, step, index], fz_recv.at[kind, step, index], to_z(step)
            )

        piece(0, pl.ds(0, main)).wait_recv()

        @pl.when(inner)
        def _():
            piece(1, pl.ds(main, 128)).wait_recv()

    def f_x(kind, step, x_at, act):
        for case, columns in ((inner, units), (first_z + last_z > 0, main)):

            @pl.when(case)
            def _(columns=columns):
                block = w3_out.at[kind, row_block(step, x_at, me_c), pl.ds(0, columns)]
                act(remote(block, block, fx_send.at[kind, step], fx_recv.at[kind, step], to_x))

    def f_x_start(kind, step):
        f_x(kind, step, me_x, lambda copy: copy.start())

    def f_x_wait(kind, step):
        f_x(kind, step, 1 - me_x, lambda copy: copy.wait_recv())

    def f_x_done(kind, step):
        f_x(kind, step, me_x, lambda copy: copy.wait_send())

    def f_c(kind, step, far):
        block = w3_out.at[kind, row_block(step, 1 - me_x if far else me_x, me_c)]
        slot = step + z_size * far
        return remote(block, block, fc_send.at[kind, slot], fc_recv.at[kind, slot], to_c)

    def f_c_in(kind, step, far):
        block = w3_out.at[kind, row_block(step, 1 - me_x if far else me_x, 1 - me_c)]
        slot = step + z_size * far
        return remote(block, block, fc_send.at[kind, slot], fc_recv.at[kind, slot], to_c)

    def d_source(step):
        return cot_hbm if isinstance(step, int) else dy_out.at[step, mine]

    def d_z_own(right):
        slot = 1 if right else z_size - 1
        return remote(
            cot_hbm, dy_out.at[slot, mine], dz_send.at[right], dz_recv.at[slot], to_z(slot)
        )

    def d_z(index):
        target, slot = hops[index]
        return remote(
            dy_out.at[order[index], mine],
            dy_out.at[slot, mine],
            dz_send.at[1 + index],
            dz_recv.at[slot],
            {"z": target},
        )

    def d_z_done():
        @pl.when(last_z == 0)
        def _():
            d_z_own(1).wait_send()

        @pl.when(first_z == 0)
        def _():
            d_z_own(0).wait_send()

        @pl.when(inner)
        def _():
            for index in range(1, z_size):
                d_z(index).wait_send()

    def d_z_in(step):
        block = dy_out.at[step, mine]
        return remote(block, block, dz_send.at[0], dz_recv.at[step], to_z(1))

    def d_y(step):
        return remote(
            d_source(step), dy_out.at[step, mine], dy_send.at[step], dy_recv.at[step], to_y
        )

    def d_y_in(step):
        block = dy_out.at[step, theirs]
        return remote(block, block, dy_send.at[step], dy_recv.at[step], to_y)

    for kind in (1, 0, 2):
        a_z_start(kind)
        a_x(kind, 0).start()
    kv_y(0, 0).start()
    tok_y.start()
    for kind in (1, 2):
        a_c(kind, 0, 0).start()

    for at_end, away in ((first_z, 1), (last_z, z_size - 1)):

        @pl.when(at_end > 0)
        def _(away=away):
            d_z_own(1 if away == 1 else 0).start()
            for kind in range(3):
                f_z(kind, away, lambda copy: copy.start())

    tok[mine, :] = tok_ref[...]
    seq = 2 * own
    query_at = lax.broadcasted_iota(jnp.int32, (seq, seq), 0)
    key_at = lax.broadcasted_iota(jnp.int32, (seq, seq), 1)
    segment = seg_ref[...].astype(jnp.float32)
    same = jnp.broadcast_to(segment, (8, seq)).T[:, :1] == segment
    allowed = same & (key_at <= query_at) & (query_at - key_at < WINDOW)
    allow_ref[...] = jnp.where(allowed, 1.0, 0.0)
    d_y(0).start()

    def pass_cotangent(index):
        d_z_in(order[index]).wait_recv()

        @pl.when(inner)
        def _():
            d_z(index).start()

        d_y(order[index]).start()

    def pass_at(at, index):
        @pl.when(me_z == at)
        def _():
            pass_cotangent(index)

    def pass_if(case, index):
        @pl.when(case)
        def _():
            pass_cotangent(index)

    outer = first_z + last_z > 0

    def from_x(index):
        step = order[index]
        for kind in (1, 0, 2):
            a_x_in(kind, step).wait_recv()
            if kind:
                a_c(kind, step, 1).start()
            else:
                kv_y(step, 1).start()

    def from_y(index):
        step = order[index]
        for far in range(2):
            kv_y_in(step, far).wait_recv()
            a_c(0, step, far).start()

    for index in range(1, z_size):
        step = order[index]
        for kind in (1, 0, 2):
            a_z_in(kind, step).wait_recv()
            a_z_next(kind, index)
            a_x(kind, step).start()
            if kind:
                a_c(kind, step, 0).start()
            else:
                kv_y(step, 0).start()
        if index == z_size - 2:

            @pl.when(inner)
            def _():
                d_z_own(1).start()
                d_z_own(0).start()

        if index == z_size - 1:
            pass_at(1, 1)
            pass_at(2, 2)
            for copy in own_f:
                copy.wait()

            @pl.when(inner)
            def _():
                for kind in range(3):
                    own_tail(kind).wait()

            for case, ways in ((inner, (1, 3, 2)), (first_z > 0, (2, 3)), (last_z > 0, (2, 1))):

                @pl.when(case)
                def _(ways=ways):
                    for away in ways:
                        for kind in range(3):
                            f_z(kind, away, lambda copy: copy.start())

            for kind in range(3):
                f_x_start(kind, 0)
                f_c(kind, 0, 0).start()
        if index >= 2:
            from_x(index - 2)
            from_y(index - 2)
    from_x(z_size - 2)
    from_y(z_size - 2)
    pass_at(1, 2)
    pass_at(2, 1)
    pass_if(outer, 1)
    from_x(z_size - 1)
    from_y(z_size - 1)

    def hand_on(kind, step):
        f_z_wait(kind, step)
        f_x_start(kind, step)
        f_c(kind, step, 0).start()

    def cross(kind, step):
        f_x_wait(kind, step)
        f_c(kind, step, 1).start()

    tok_y_in.wait_recv()
    own_q.wait()
    own_o.wait()
    for kind in (0, 1):
        for step in range(z_size):
            for far in range(2):
                a_c_in(kind, step, far).wait_recv()

    gains = kv_w[:, 2 * head :].astype(jnp.float32).T[:8, :]
    gain_ref[...] = gains

    def norm_rows(index, carry):
        at = pl.ds(pl.multiple_of(index * 32, 32), 32)
        values = tok[at, :].astype(jnp.float32)
        scale = lax.rsqrt(jnp.mean(values * values, axis=-1, keepdims=True) + epsilon)
        n1_ref[at, :] = (values * scale * gain_ref[0:1, :]).astype(jnp.bfloat16)
        return carry

    lax.fori_loop(0, 2 * own // 32, norm_rows, 0)
    pass_if(inner, 3)
    hand_on(0, order[1])
    hand_on(1, order[1])
    table = (cos_ref[...], sin_ref[...])
    key_ref[...] = spin(dot_nn(n1_ref[...], kv_w[:, :head]), table).astype(jnp.bfloat16)
    val_ref[...] = dot_nn(n1_ref[...], kv_w[:, head : 2 * head]).astype(jnp.bfloat16)
    head_scale = head ** (-0.5)
    heads = att_ref.shape[1] // head

    half_cols = att_ref.shape[1] // 2
    for index in range(2):
        cols = pl.ds(index * half_cols, half_cols)
        query[:, cols] = dot_nn(n1_ref[...], q_w[:, cols])

    def attend(index):
        cols = pl.ds(index * head, head)
        rotated = (spin(query[:, cols], table) * head_scale).astype(jnp.bfloat16)
        rot_ref[:, cols] = rotated
        probs = head_probs(rotated, key_ref[...], allow_ref[...]).astype(jnp.bfloat16)
        att_ref[:, cols] = dot_nn(probs, val_ref[...]).astype(jnp.bfloat16)

    tasks = [
        lambda: hand_on(2, order[1]),
        lambda: cross(0, 0),
        lambda: hand_on(0, order[2]),
        lambda: cross(1, 0),
        lambda: (hand_on(1, order[2]), cross(2, 0)),
    ]
    for index in range(heads):
        attend(index)
        if index < len(tasks):
            tasks[index]()
    for step in range(z_size):
        for far in range(2):
            a_c_in(2, step, far).wait_recv()
    saves = [
        local(kv_w, kv_out),
        local(q_w, wq_out),
        local(o_w, wo_out),
    ]
    span = width // 4

    def project(index, carry):
        cols = pl.ds(pl.multiple_of(index * span, span), span)
        part[:, cols] = matmul_nt(att_ref[...], o_w[cols, :]).astype(jnp.bfloat16)
        return carry

    lax.fori_loop(0, 4, project, 0)
    part_out.start()
    hand_on(2, order[2])
    cross(0, order[1])
    cross(1, order[1])
    pass_if(outer, 2)
    part_out.wait_recv()

    def middle(index, carry):
        at = pl.ds(pl.multiple_of(index * 32, 32), 32)
        there = pl.ds(pl.multiple_of(me_y * own + index * 32, 32), 32)
        values = (
            tok_ref[at, :].astype(jnp.float32)
            + part[there, :].astype(jnp.float32)
            + part_y[at, :].astype(jnp.float32)
        )
        mid_ref[at, :] = values
        scale = lax.rsqrt(jnp.mean(values * values, axis=-1, keepdims=True) + epsilon)
        n2_ref[there, :] = (values * scale * gain_ref[1:2, :]).astype(jnp.bfloat16)
        return carry

    lax.fori_loop(0, own // 32, middle, 0)
    n2_y.start()
    hand_on(0, order[3])
    cross(2, order[1])
    cross(0, order[2])
    pass_if(outer, 3)
    hand_on(1, order[3])
    cross(1, order[2])
    hand_on(2, order[3])
    cross(2, order[2])
    for kind in range(3):
        cross(kind, order[3])
    for kind in range(3):
        for step in range(z_size):
            for far in range(2):
                f_c_in(kind, step, far).wait_recv()
    for step in range(z_size):
        d_y_in(step).wait_recv()
    n2_y_in.wait_recv()

    for kind in range(3):
        a_z_done(kind)
    d_z_done()
    tok_y.wait_send()
    part_out.wait_send()
    n2_y.wait_send()
    own_d.wait()
    for copy in saves:
        copy.wait()
    for step in range(z_size):
        d_y(step).wait_send()
        for far in range(2):
            kv_y(step, far).wait_send()
        for kind in range(3):
            if step:
                f_z(kind, step, lambda copy: copy.wait_send())
            a_x(kind, step).wait_send()
            f_x_done(kind, step)
            for far in range(2):
                a_c(kind, step, far).wait_send()
                f_c(kind, step, far).wait_send()


def pre_call(
    tokens, w_kv, gain_one, gain_two, table, segments, cotangent, w_query, w_out, ffn
):
    z_size = lax.axis_size("z")
    own, width = tokens.shape
    seq = 2 * own
    rows, cols = w_query.shape
    head = table[0].shape[1] * 2
    units = ragged_split(ffn[0].shape[1], z_size)[1]
    low = lambda *dims: jax.ShapeDtypeStruct(dims, jnp.bfloat16)
    full = lambda *dims: jax.ShapeDtypeStruct(dims, jnp.float32)
    dma = lambda *lead: pltpu.SemaphoreType.DMA(lead)
    vmem = pl.BlockSpec(memory_space=pltpu.VMEM)
    hbm = pl.BlockSpec(memory_space=pl.ANY)
    wide = lambda *lead: pltpu.VMEM((*lead, width), jnp.bfloat16)
    return pl.pallas_call(
        functools.partial(pre_kernel, z_size),
        out_shape=(
            low(seq, width),
            low(seq, cols),
            low(seq, head),
            low(seq, head),
            low(seq, cols),
            full(own, width),
            low(seq, width),
            full(8, width),
            full(seq, seq),
            low(width, 2 * head + 128),
            low(width, cols),
            low(width, cols),
            low(3, width, units),
            low(z_size, seq, width),
        ),
        in_specs=[vmem] * 7 + [hbm] * 6,
        out_specs=(vmem,) * 9 + (hbm,) * 5,
        scratch_shapes=[
            pltpu.VMEM((width, 2 * head + 128), jnp.bfloat16),
            pltpu.VMEM((width, cols), jnp.bfloat16),
            pltpu.VMEM((width, cols), jnp.bfloat16),
            wide(seq),
            wide(seq),
            wide(own),
            pltpu.VMEM((seq, cols), jnp.float32),
            pltpu.VMEM((128, 128), jnp.float32),
            dma(4),
            dma(4),
            dma(2 * z_size),
            dma(2 * z_size),
            dma(3, z_size + 1),
            dma(3, z_size),
            dma(3, z_size),
            dma(3, z_size),
            dma(3, 2 * z_size),
            dma(3, 2 * z_size),
            dma(3, z_size, 2),
            dma(3, z_size, 2),
            dma(3, z_size),
            dma(3, z_size),
            dma(3, 2 * z_size),
            dma(3, 2 * z_size),
            dma(z_size + 1),
            dma(z_size),
            dma(z_size),
            dma(z_size),
            dma(16),
        ],
        compiler_params=pltpu.CompilerParams(
            collective_id=1, has_side_effects=True, vmem_limit_bytes=VMEM_BYTES
        ),
        cost_estimate=pl.CostEstimate(
            flops=8 * seq * width * cols,
            bytes_accessed=8 * width * (cols + units),
            transcendentals=seq * seq * cols // head,
        ),
    )(tokens, w_kv, gain_one, gain_two, *table, segments, cotangent, w_query, w_out, *ffn)


def post_kernel(
    z_size,
    main,
    tok_ref,
    gain_ref,
    gain_part_ref,
    n1_ref,
    rot_ref,
    key_ref,
    val_ref,
    att_ref,
    cos_ref,
    sin_ref,
    allow_ref,
    kv_hbm,
    wq_hbm,
    wo_hbm,
    mix_hbm,
    gmf_hbm,
    gmb_hbm,
    mid_hbm,
    sums_hbm,
    mixed_ref,
    tgrad_ref,
    gsum_ref,
    kvg_ref,
    qg_ref,
    og_ref,
    ffn_out,
    kv_w,
    q_w,
    o_w,
    o_part,
    gm,
    gm_f,
    gq,
    gkv,
    kv_sum,
    back_y,
    mix_y,
    mix_z,
    mix_s,
    o_c,
    o_x,
    o_z,
    q_c,
    q_x,
    q_z,
    kv_y,
    kv_c,
    kv_x,
    kv_z,
    gain_own,
    gain_in,
    ffn_in,
    ffn_own,
    load_sem,
    own_sem,
    fx_send,
    fx_recv,
    fz_send,
    fz_recv,
    y_send,
    y_recv,
    my_send,
    my_recv,
    mz_send,
    mz_recv,
    wc_send,
    wc_recv,
    wx_send,
    wx_recv,
    wz_send,
    wz_recv,
    kc_send,
    kc_recv,
    kz_send,
    kz_recv,
    g_send,
    g_recv,
):
    me_z, me_x = lax.axis_index("z"), lax.axis_index("x")
    me_c, me_y = lax.axis_index("c"), lax.axis_index("mp")
    own, width = tok_ref.shape
    seq = 2 * own
    head = key_ref.shape[1]
    cols_here = att_ref.shape[1]
    heads = cols_here // head
    rows = qg_ref.shape[0]
    span = width // z_size
    mine = pl.ds(pl.multiple_of(me_y * own, own), own)
    theirs = pl.ds(pl.multiple_of((1 - me_y) * own, own), own)
    to_y, to_x, to_c = {"mp": 1 - me_y}, {"x": 1 - me_x}, {"c": 1 - me_c}
    head_scale = head ** (-0.5)

    def behind(step):
        return lax.rem(me_z - step + z_size, z_size)

    def to_z(step):
        return {"z": lax.rem(me_z + step, z_size)}

    def row_block(step, x_at, c_at):
        start = ((behind(step) * 2 + x_at) * 2 + c_at) * rows
        return pl.ds(pl.multiple_of(start, rows), rows)

    loads = [
        pltpu.make_async_copy(wo_hbm, o_w, load_sem.at[0]),
        pltpu.make_async_copy(wq_hbm, q_w, load_sem.at[1]),
        pltpu.make_async_copy(
            kv_hbm.at[:, :, :, :, :, pl.ds(0, 2 * head)], kv_w, load_sem.at[2]
        ),
    ]
    for step in range(z_size):
        loads.append(
            pltpu.make_async_copy(mix_hbm.at[step, me_y], mix_s.at[step], load_sem.at[3 + step])
        )
    loads.append(pltpu.make_async_copy(gmf_hbm, gm_f, load_sem.at[3 + z_size]))
    loads.append(pltpu.make_async_copy(gmb_hbm, gm.at[mine], load_sem.at[4 + z_size]))
    mid_load = pltpu.make_async_copy(mid_hbm, gm_f, load_sem.at[5 + z_size])
    for load in loads:
        load.start()

    barrier = pltpu.get_barrier_semaphore()
    peers = [to_y, to_x, to_c] + [to_z(step) for step in range(1, z_size)]
    for where in peers:
        pl.semaphore_signal(barrier, inc=1, device_id=where, device_id_type=MESH_ID)
    pl.semaphore_wait(barrier, len(peers))

    tasks = [(step, kind) for step in (2, 3) for kind in range(3)]

    def f_x(index):
        step, kind = tasks[index]
        return remote(
            sums_hbm.at[kind, step, 1],
            ffn_in.at[index],
            fx_send.at[index],
            fx_recv.at[index],
            to_x,
        )

    def f_own(index):
        step, kind = tasks[index]
        return pltpu.make_async_copy(
            sums_hbm.at[kind, step, 0], ffn_own.at[index % 2], own_sem.at[index % 2]
        )

    def f_z(step, kind, source_z, act):
        for case, columns in (
            ((source_z > 0) & (source_z < z_size - 1), ffn_out.shape[3]),
            ((source_z == 0) | (source_z == z_size - 1), main),
        ):

            @pl.when(case)
            def _(columns=columns):
                cols = pl.ds(0, columns)
                if step == 1:
                    src = sums_hbm.at[kind, 1, 0, :, cols]
                else:
                    src = ffn_in.at[tasks.index((step, kind)), :, cols]
                act(
                    remote(
                        src,
                        ffn_out.at[kind, step, :, cols],
                        fz_send.at[kind, step],
                        fz_recv.at[kind, step],
                        to_z(step),
                    )
                )

    def tick(index):
        step, kind = tasks[index]
        f_x(index).wait_recv()
        f_own(index).wait()
        block = ffn_in.at[index]
        add_rows(block, [ffn_own.at[index % 2]], block, rows)
        if index + 2 < len(tasks):
            f_own(index + 2).start()
        f_z(step, kind, me_z, lambda copy: copy.start())

    def f_x_own(kind):
        return remote(
            sums_hbm.at[kind, 0, 1],
            ffn_out.at[kind, 0],
            fx_send.at[len(tasks) + kind],
            fx_recv.at[len(tasks) + kind],
            to_x,
        )

    f_own(0).start()
    f_own(1).start()
    for index in range(len(tasks)):
        f_x(index).start()
    for kind in range(3):
        f_z(1, kind, me_z, lambda copy: copy.start())

    gm_y = remote(gmb_hbm, gm.at[mine], y_send.at[0], y_recv.at[0], to_y)
    gm_y_in = remote(gm.at[theirs], gm.at[theirs], y_send.at[0], y_recv.at[0], to_y)
    gm_y.start()

    first_z, last_z = (z_size - 1 - me_z) // (z_size - 1), me_z // (z_size - 1)
    inner = first_z + last_z == 0
    order = (
        0,
        1 + (me_z + 1) // 2,
        2 + (2 * me_z - 3) * (1 - first_z - last_z),
        3 - 2 * (me_z // 2),
    )
    right = (None, 1 - me_z // 2, (3 - me_z) * (2 - me_z) // 6 + me_z // 2 * (1 - last_z), 1 - me_z // 2)

    def hop_slot(index):
        step, way = order[index], right[index]
        return way * lax.rem(step + 1, z_size) + (1 - way) * (step - 1 + 4 * ((3 - step) // 2))

    def hop_target(index):
        return {"z": me_z + 2 * right[index] - 1}

    def mix_over_y(step):
        return remote(
            mix_hbm.at[step, 1 - me_y], mix_y.at[step], my_send.at[step], my_recv.at[step], to_y
        )

    def mix_over_z(index):
        slot = hop_slot(index)
        return remote(
            mix_s.at[order[index]],
            mix_z.at[slot],
            mz_send.at[index],
            mz_recv.at[slot],
            hop_target(index),
        )

    def mix_z_in(slot):
        return remote(mix_z.at[slot], mix_z.at[slot], mz_send.at[1], mz_recv.at[slot], to_z(1))

    def mix_add(step, others, last):
        def add_tile(tile, carry):
            at = pl.ds(pl.multiple_of(tile * TILE, TILE), TILE)
            total = mix_s[step, at, :].astype(jnp.float32)
            for other in others:
                total = total + other[at, :].astype(jnp.float32)
            if last:
                mixed_ref[:, at] = (gm_f[:, at] + total.T).astype(jnp.bfloat16)
            else:
                mix_s[step, at, :] = total.astype(jnp.bfloat16)
            return carry

        lax.fori_loop(0, width // TILE, add_tile, 0)

    def mix_step(index):
        step = order[index]
        mix_over_y(step).wait_recv()
        from_y = mix_y.at[step]
        if index:

            @pl.when(inner)
            def _():
                mix_z_in(step).wait_recv()
                mix_add(step, [from_y, mix_z.at[step]], False)

            @pl.when(first_z + last_z > 0)
            def _():
                mix_add(step, [from_y], False)

            mix_over_z(index).start()
        else:
            mid_load.wait()

            @pl.when(first_z == 0)
            def _():
                mix_z_in(0).wait_recv()

            @pl.when(last_z == 0)
            def _():
                mix_z_in(z_size).wait_recv()

            @pl.when(inner)
            def _():
                mix_add(0, [from_y, mix_z.at[0], mix_z.at[z_size]], True)

            @pl.when(first_z > 0)
            def _():
                mix_add(0, [from_y, mix_z.at[z_size]], True)

            @pl.when(last_z > 0)
            def _():
                mix_add(0, [from_y, mix_z.at[0]], True)

    for index in (1, 2, 3, 0):
        mix_over_y(order[index]).start()

    kinds = ((o_part, o_c, o_x, o_z, og_ref), (o_w, q_c, q_x, q_z, qg_ref))

    def w_c(kind, step, far):
        x_at = 1 - me_x if far else me_x
        return remote(
            kinds[kind][0].at[row_block(step, x_at, 1 - me_c)],
            kinds[kind][1].at[step, far],
            wc_send.at[kind, step, far],
            wc_recv.at[kind, step, far],
            to_c,
        )

    def w_x(kind, step):
        return remote(
            kinds[kind][0].at[row_block(step, 1 - me_x, me_c)],
            kinds[kind][2].at[step],
            wx_send.at[kind, step],
            wx_recv.at[kind, step],
            to_x,
        )

    def w_z(kind, index):
        step, slot = order[index], hop_slot(index)
        return remote(
            kinds[kind][0].at[row_block(step, me_x, me_c)],
            kinds[kind][3].at[slot],
            wz_send.at[kind, index],
            wz_recv.at[kind, slot],
            hop_target(index),
        )

    def w_z_in(kind, slot):
        block = kinds[kind][3].at[slot]
        return remote(block, block, wz_send.at[kind, 1], wz_recv.at[kind, slot], to_z(1))

    def w_x_stage(kind, index):
        step = order[index]
        w_c(kind, step, 1).wait_recv()
        block = kinds[kind][0].at[row_block(step, 1 - me_x, me_c)]
        add_rows(block, [kinds[kind][1].at[step, 1]], block, rows)
        w_x(kind, step).start()

    def w_z_stage(kind, index):
        part, from_c, from_x, from_z, result = kinds[kind]
        step = order[index]
        w_c(kind, step, 0).wait_recv()
        w_x(kind, step).wait_recv()
        block = part.at[row_block(step, me_x, me_c)]
        others = [from_c.at[step, 0], from_x.at[step]]
        if index:

            @pl.when(inner)
            def _():
                w_z_in(kind, step).wait_recv()
                add_rows(block, [*others, from_z.at[step]], block, rows)

            @pl.when(first_z + last_z > 0)
            def _():
                add_rows(block, others, block, rows)

            w_z(kind, index).start()
        else:

            @pl.when(first_z == 0)
            def _():
                w_z_in(kind, 0).wait_recv()

            @pl.when(last_z == 0)
            def _():
                w_z_in(kind, z_size).wait_recv()

            @pl.when(inner)
            def _():
                add_rows(block, [*others, from_z.at[0], from_z.at[z_size]], result, rows)

            @pl.when(first_z > 0)
            def _():
                add_rows(block, [*others, from_z.at[z_size]], result, rows)

            @pl.when(last_z > 0)
            def _():
                add_rows(block, [*others, from_z.at[0]], result, rows)

    def w_product(kind, index, left, values):
        step = order[index]
        at = pl.ds(pl.multiple_of(behind(step) * span, 128), span)
        turned = left[:, at].T

        def tile_body(tile, carry):
            cols = pl.ds(pl.multiple_of(tile * TILE, TILE), TILE)
            kinds[kind][0][at, cols] = dot_nn(turned, values[:, cols]).astype(jnp.bfloat16)
            return carry

        lax.fori_loop(0, cols_here // TILE, tile_body, 0)
        for far in (1, 0):
            w_c(kind, step, far).start()

    tick(0)
    tick(1)
    loads[-1].wait()
    gm_y_in.wait_recv()
    w_product(0, 1, gm, att_ref)
    w_product(0, 2, gm, att_ref)
    w_x_stage(0, 1)
    w_product(0, 3, gm, att_ref)
    w_x_stage(0, 2)
    tick(2)
    w_product(0, 0, gm, att_ref)
    w_x_stage(0, 3)
    for load in loads[:-1]:
        load.wait()

    kv_sum[...] = jnp.zeros(kv_sum.shape, jnp.float32)
    table = (cos_ref[...], sin_ref[...])

    for index in range(2):
        cols = pl.ds(index * (cols_here // 2), cols_here // 2)
        gq[:, cols] = dot_nn(gm[...], o_w[:, cols]).astype(jnp.bfloat16)

    def attend_back(index):
        cols = pl.ds(index * head, head)
        grad_vals = gq[:, cols]
        rotated = rot_ref[:, cols]
        probs = head_probs(rotated, key_ref[...], allow_ref[...])
        grad_probs = matmul_nt(grad_vals, val_ref[...])
        delta = jnp.sum(probs * grad_probs, axis=-1, keepdims=True)
        grad_scores = (probs * (grad_probs - delta)).astype(jnp.bfloat16)
        grad_rot = dot_nn(grad_scores, key_ref[...])
        gq[:, cols] = (spin_back(grad_rot, table) * head_scale).astype(jnp.bfloat16)
        kv_sum[0] += matmul_tn(grad_scores, rotated)
        kv_sum[1] += matmul_tn(probs.astype(jnp.bfloat16), grad_vals)

    for index in range(heads):
        attend_back(index)
        if index == 0:
            w_x_stage(0, 0)
        if 3 + index < len(tasks):
            tick(3 + index)
        if index == heads - 1:
            mix_step(1)
    gkv[:, :head] = spin_back(kv_sum[0], table).astype(jnp.bfloat16)
    gkv[:, head:] = kv_sum[1].astype(jnp.bfloat16)

    w_product(1, 1, n1_ref, gq)
    w_product(1, 2, n1_ref, gq)
    w_x_stage(1, 1)
    w_z_stage(0, 1)
    w_product(1, 3, n1_ref, gq)
    w_x_stage(1, 2)
    w_product(1, 0, n1_ref, gq)
    w_x_stage(1, 3)
    w_x_stage(1, 0)
    for kind in range(3):
        f_x_own(kind).start()

    gm_y.wait_send()
    back = gm
    def input_tile(index, carry):
        at = pl.ds(pl.multiple_of(index * span, 128), span)
        back[:, at] = (
            matmul_nt(gq[...], q_w[at, :]) + matmul_nt(gkv[...], kv_w[index].reshape(span, 2 * head))
        ).astype(jnp.bfloat16)
        return carry

    lax.fori_loop(0, z_size, input_tile, 0)
    back_out = remote(back.at[theirs], back_y, y_send.at[1], y_recv.at[1], to_y)
    back_out.start()

    kv_part = kv_w

    def kv_tile(index, carry):
        at = pl.ds(pl.multiple_of(index * span, 128), span)
        product = dot_nn(n1_ref[:, at].T, gkv[...]).astype(jnp.bfloat16)
        kv_part[index] = product.reshape(kv_part.shape[1:])
        return carry

    lax.fori_loop(0, z_size, kv_tile, 0)
    kv_over_y = remote(kv_part.at[:, :, :, 1 - me_y], kv_y, y_send.at[2], y_recv.at[2], to_y)
    kv_over_y.start()
    mix_step(2)
    w_z_stage(0, 2)
    mix_step(3)
    w_z_stage(0, 3)

    back_out.wait_recv()

    def input_rows(index, total):
        at = pl.ds(pl.multiple_of(index * 32, 32), 32)
        there = pl.ds(pl.multiple_of(me_y * own + index * 32, 32), 32)
        upstream = back[there, :].astype(jnp.float32) + back_y[at, :].astype(jnp.float32)
        grad, gain_part = norm_back(
            tok_ref[at, :].astype(jnp.float32), gain_ref[0:1, :], upstream
        )
        tgrad_ref[at, :] = (gm_f[at, :] + grad).astype(jnp.bfloat16)
        return total + gain_part

    attn_gain_part = lax.fori_loop(
        0, own // 32, input_rows, jnp.zeros((1, width), jnp.float32)
    )
    for index in range(4):
        at = slice(index * span, (index + 1) * span)
        gain_own[0, index : index + 1, :] = attn_gain_part[:, at]
        gain_own[0, 4 + index : 5 + index, :] = gain_part_ref[4 + index : 5 + index, :]

    def gain_send(stage, where):
        return remote(
            gain_own.at[stage], gain_in.at[stage], g_send.at[stage], g_recv.at[stage], where
        )

    gain_hops = [gain_send(0, to_y), gain_send(1, to_c), gain_send(2, to_x)]
    gain_last = [
        remote(
            gain_own.at[3], gain_in.at[2 + step], g_send.at[2 + step], g_recv.at[2 + step], to_z(step)
        )
        for step in range(1, z_size)
    ]

    def gain_fold(stage):
        gain_hops[stage].wait_recv()
        gain_own[stage + 1] = gain_own[stage] + gain_in[stage]

    gain_hops[0].start()
    mid_load.start()
    w_z_stage(1, 1)
    w_z_stage(0, 0)
    w_z_stage(1, 2)
    gain_fold(0)
    gain_hops[1].start()
    mix_step(0)
    w_z_stage(1, 3)
    gain_fold(1)
    gain_hops[2].start()
    kv_over_y.wait_recv()

    def kv_add_y(index, carry):
        for x_at in range(2):
            for c_at in range(2):
                block = kv_part.at[index, x_at, c_at, me_y]
                block[...] = (
                    block[...].astype(jnp.float32) + kv_y[index, x_at, c_at].astype(jnp.float32)
                ).astype(jnp.bfloat16)
        return carry

    lax.fori_loop(0, z_size, kv_add_y, 0)
    kv_over_c = remote(
        kv_part.at[:, :, 1 - me_c, me_y], kv_c, kc_send.at[0], kc_recv.at[0], to_c
    )
    kv_over_c.start()
    gain_fold(2)
    for copy in gain_last:
        copy.start()
    kv_over_c.wait_recv()

    def kv_add_c(index, carry):
        for x_at in range(2):
            block = kv_part.at[index, x_at, me_c, me_y]
            block[...] = (
                block[...].astype(jnp.float32) + kv_c[index, x_at].astype(jnp.float32)
            ).astype(jnp.bfloat16)
        return carry

    lax.fori_loop(0, z_size, kv_add_c, 0)
    kv_over_x = remote(
        kv_part.at[:, 1 - me_x, me_c, me_y], kv_x, kc_send.at[1], kc_recv.at[1], to_x
    )
    kv_over_x.start()
    w_z_stage(1, 0)
    kv_over_x.wait_recv()

    def kv_add_x(index, carry):
        block = kv_part.at[index, me_x, me_c, me_y]
        block[...] = (
            block[...].astype(jnp.float32) + kv_x[index].astype(jnp.float32)
        ).astype(jnp.bfloat16)
        return carry

    lax.fori_loop(0, z_size, kv_add_x, 0)
    kv_over_z = [
        remote(
            kv_part.at[lax.rem(me_z + step, z_size), me_x, me_c, me_y],
            kv_z.at[step - 1],
            kz_send.at[step],
            kz_recv.at[step],
            to_z(step),
        )
        for step in range(1, z_size)
    ]
    for copy in kv_over_z:
        copy.start()
    for copy in gain_last:
        copy.wait_recv()
    gsum_ref[...] = gain_own[3] + gain_in[3] + gain_in[4] + gain_in[5]
    for copy in kv_over_z:
        copy.wait_recv()
    kvg_ref[...] = (
        kv_part[me_z, me_x, me_c, me_y].astype(jnp.float32)
        + kv_z[0].astype(jnp.float32)
        + kv_z[1].astype(jnp.float32)
        + kv_z[2].astype(jnp.float32)
    )

    back_out.wait_send()
    kv_over_y.wait_send()
    kv_over_c.wait_send()
    kv_over_x.wait_send()
    for kind in range(3):
        f_x_own(kind).wait()
    for index in range(len(tasks)):
        f_x(index).wait_send()
    for step in range(1, z_size):
        for kind in range(3):
            f_z(step, kind, me_z, lambda copy: copy.wait_send())
            f_z(step, kind, behind(step), lambda copy: copy.wait_recv())
    for copy in gain_hops + gain_last + kv_over_z:
        copy.wait_send()
    for step in range(z_size):
        mix_over_y(step).wait_send()
        if step:
            mix_over_z(step).wait_send()
        for kind in range(2):
            w_c(kind, step, 0).wait_send()
            w_c(kind, step, 1).wait_send()
            w_x(kind, step).wait_send()
            if step:
                w_z(kind, step).wait_send()


def post_call(
    tokens,
    gains,
    gain_part,
    normed_one,
    rotated,
    keys,
    values,
    attn_vals,
    table,
    allowed,
    kv_weight,
    query_weight,
    out_weight,
    mix_parts,
    grad_mid,
    grad_mid_low,
    mid,
    ffn_sums,
    main,
):
    z_size = lax.axis_size("z")
    own, width = tokens.shape
    seq = 2 * own
    head = keys.shape[1]
    cols = attn_vals.shape[1]
    rows = width // (4 * z_size)
    units = ffn_sums.shape[4]
    low = lambda *dims: pltpu.VMEM(dims, jnp.bfloat16)
    full = lambda *dims: pltpu.VMEM(dims, jnp.float32)
    out_full = lambda *dims: jax.ShapeDtypeStruct(dims, jnp.float32)
    out_low = lambda *dims: jax.ShapeDtypeStruct(dims, jnp.bfloat16)
    dma = lambda *lead: pltpu.SemaphoreType.DMA(lead)
    vmem = pl.BlockSpec(memory_space=pltpu.VMEM)
    hbm = pl.BlockSpec(memory_space=pl.ANY)
    z = z_size
    return pl.pallas_call(
        functools.partial(post_kernel, z_size, main),
        out_shape=(
            out_low(own, width),
            out_low(own, width),
            out_full(8, width // z),
            out_full(rows // 2, 2 * head),
            out_full(rows, cols),
            out_full(rows, cols),
            out_low(3, z, rows, units),
        ),
        in_specs=[vmem] * 11 + [hbm] * 8,
        out_specs=(vmem,) * 6 + (hbm,),
        scratch_shapes=[
            low(z, 2, 2, 2, rows // 2, 2 * head),
            low(width, cols),
            low(width, cols),
            low(width, cols),
            low(seq, width),
            full(own, width),
            low(seq, cols),
            low(seq, 2 * head),
            full(2, seq, head),
            low(own, width),
            low(z, width, own),
            low(z + 1, width, own),
            low(z, width, own),
            low(z, 2, rows, cols),
            low(z, rows, cols),
            low(z + 1, rows, cols),
            low(z, 2, rows, cols),
            low(z, rows, cols),
            low(z + 1, rows, cols),
            low(z, 2, 2, rows // 2, 2 * head),
            low(z, 2, rows // 2, 2 * head),
            low(z, rows // 2, 2 * head),
            low(z - 1, rows // 2, 2 * head),
            full(4, 8, width // z),
            full(6, 8, width // z),
            low(6, rows, units),
            low(2, rows, units),
            dma(6 + z),
            dma(2),
            dma(9),
            dma(9),
            dma(3, z),
            dma(3, z),
            dma(3),
            dma(3),
            dma(z),
            dma(z),
            dma(z),
            dma(z + 1),
            dma(2, z, 2),
            dma(2, z, 2),
            dma(2, z),
            dma(2, z),
            dma(2, z),
            dma(2, z + 1),
            dma(2),
            dma(2),
            dma(z),
            dma(z),
            dma(6),
            dma(6),
        ],
        compiler_params=pltpu.CompilerParams(
            collective_id=2, has_side_effects=True, vmem_limit_bytes=VMEM_BYTES
        ),
        cost_estimate=pl.CostEstimate(
            flops=14 * seq * width * cols,
            bytes_accessed=10 * width * cols,
            transcendentals=seq * seq * cols // head,
        ),
    )(
        tokens,
        gains,
        gain_part,
        normed_one,
        rotated,
        keys,
        values,
        attn_vals,
        *table,
        allowed,
        kv_weight.reshape(z, 2, 2, 2, rows // 2, kv_weight.shape[1]),
        query_weight,
        out_weight,
        mix_parts,
        grad_mid,
        grad_mid_low,
        mid,
        ffn_sums,
    )


def layout_kernel(
    z_size,
    main,
    sum_ref,
    ffn_ref,
    q_ref,
    o_ref,
    kv_ref,
    mixed_in,
    tgrad_in,
    wg_ref,
    wu_ref,
    wd_ref,
    qg_ref,
    og_ref,
    kvg_ref,
    mixed_ref,
    tgrad_ref,
):
    me_z = lax.axis_index("z")
    for kind, out in enumerate((wg_ref, wu_ref, wd_ref)):
        for step in range(z_size):
            at = lax.rem(me_z - step + z_size, z_size)
            values = ffn_ref[kind, step].astype(jnp.float32)
            if step == 0:
                values = values + sum_ref[kind, 0, 0].astype(jnp.float32)
            body = pl.ds(pl.multiple_of(at * main, 128), main)
            out[:, body] = values[:, :main]

            @pl.when((at > 0) & (at < z_size - 1))
            def _(out=out, at=at, values=values):
                tail = z_size * main + lax.rem(at + 1, 2) * 128
                out[:, pl.ds(pl.multiple_of(tail, 128), 128)] = values[:, main:]
    qg_ref[...] = q_ref[...]
    og_ref[...] = o_ref[...]
    kvg_ref[...] = kv_ref[...]
    mixed_ref[...] = mixed_in[...]
    tgrad_ref[...] = tgrad_in[...]


def layout_call(ffn_sums, ffn_grads, query_grad, out_grad, kv_grad, mixed, tokens_grad, ffn_cols):
    z_size = lax.axis_size("z")
    main, units = ragged_split(ffn_cols, z_size)
    rows, cols = query_grad.shape
    parts = rows // 80
    kv_rows = kv_grad.shape[0] // parts
    full = lambda *dims: jax.ShapeDtypeStruct(dims, jnp.float32)
    row = lambda height, width: pl.BlockSpec((height, width), lambda index: (index, 0))
    own, width = mixed.shape
    share = pl.BlockSpec((own, width // parts), lambda index: (0, index))
    specs = [row(80, cols), row(80, cols), row(kv_rows, kv_grad.shape[1]), share, share]
    return pl.pallas_call(
        functools.partial(layout_kernel, z_size, main),
        grid=(parts,),
        out_shape=(
            *[full(rows, ffn_cols)] * 3,
            full(rows, cols),
            full(rows, cols),
            full(*kv_grad.shape),
            jax.ShapeDtypeStruct(mixed.shape, jnp.bfloat16),
            jax.ShapeDtypeStruct(mixed.shape, jnp.bfloat16),
        ),
        in_specs=[
            pl.BlockSpec((3, 1, 1, 80, units), lambda index: (0, 0, 0, index, 0)),
            pl.BlockSpec((3, z_size, 80, units), lambda index: (0, 0, index, 0)),
            *specs,
        ],
        out_specs=(*[row(80, ffn_cols)] * 3, *specs),
        compiler_params=pltpu.CompilerParams(vmem_limit_bytes=VMEM_BYTES),
    )(ffn_sums, ffn_grads, query_grad, out_grad, kv_grad, mixed, tokens_grad)


FF_SPLIT = 4


def ffn_pass(normed, grad_out, gate_weight, up_weight, down_weight):
    gate = jnp.dot(normed, gate_weight, preferred_element_type=jnp.float32)
    up_proj = jnp.dot(normed, up_weight, preferred_element_type=jnp.float32)
    grad_hidden = jnp.dot(grad_out, down_weight, preferred_element_type=jnp.float32)
    product, pull = jax.vjp(gelu_product, gate, up_proj)
    hidden = product.astype(jnp.bfloat16)
    grad_gate_f, grad_up_f = pull(grad_hidden)
    grad_gate = grad_gate_f.astype(jnp.bfloat16)
    grad_up = grad_up_f.astype(jnp.bfloat16)
    mixed_part = matmul_nt(hidden, down_weight).astype(jnp.bfloat16)
    normed_part = (matmul_nt(grad_gate, gate_weight) + matmul_nt(grad_up, up_weight)).astype(
        jnp.bfloat16
    )
    weight_parts = [
        matmul_tn(normed, grad_gate).astype(jnp.bfloat16),
        matmul_tn(normed, grad_up).astype(jnp.bfloat16),
        matmul_tn(grad_out, hidden).astype(jnp.bfloat16),
    ]
    return mixed_part, normed_part, weight_parts


def shards_general(
    tokens,
    segments,
    positions,
    cotangent,
    attn_gain,
    ffn_gain,
    w_kv,
    w_query,
    w_out,
    w_gate,
    w_up,
    w_down,
):
    everywhere = ("z", "xc", "mp")
    dp = ("z", "xc")
    z_size = lax.axis_size("z")
    xc_size = lax.axis_size("xc")
    gains = lax.all_gather(
        jnp.stack([attn_gain, ffn_gain], axis=1), everywhere, axis=0, tiled=True
    ).astype(jnp.float32)
    gain_one, gain_two = gains[:, 0], gains[:, 1]
    kv_weight = lax.all_gather(w_kv, everywhere, axis=0, tiled=True)
    head_dim = kv_weight.shape[1] // 2
    width = tokens.shape[1]
    seq_len = segments.shape[0]
    heads_here = w_query.shape[1] // head_dim
    scale = head_dim ** (-0.5)
    cosine, sine = rotary_angles(positions, head_dim)
    inputs_f = tokens.astype(jnp.float32)
    tokens_all = lax.all_gather(tokens, "mp", axis=0, tiled=True)
    normed_one = norm_gain(tokens_all.astype(jnp.float32), gain_one).astype(jnp.bfloat16)
    query_weight = lax.all_gather(w_query, dp, axis=0, tiled=True)
    out_weight = lax.all_gather(w_out, dp, axis=0, tiled=True)

    rows = w_gate.shape[0]
    unit = w_gate.shape[1] // z_size

    def spread(weight):
        pieces = weight.reshape(rows, z_size, unit).transpose(1, 0, 2)
        pieces = lax.all_to_all(pieces, "z", split_axis=0, concat_axis=0, tiled=True)
        return lax.all_gather(pieces, "xc", axis=1, tiled=False).reshape(width, unit)

    gate_weight, up_weight, down_weight = spread(w_gate), spread(w_up), spread(w_down)
    grad_all = lax.all_gather(cotangent, ("z", "mp"), axis=0, tiled=True)

    query = jnp.dot(normed_one, query_weight, preferred_element_type=jnp.float32).reshape(
        seq_len, heads_here, head_dim
    )
    rotated = (rotate(query, cosine[:, None], sine[:, None]) * scale).astype(jnp.bfloat16)
    keyval = jnp.dot(normed_one, kv_weight, preferred_element_type=jnp.float32)
    keys = rotate(keyval[:, :head_dim], cosine, sine).astype(jnp.bfloat16)
    values = keyval[:, head_dim:].astype(jnp.bfloat16)
    allowed = block_allowed(segments, 0, seq_len)
    scores = jnp.einsum("thd,sd->hts", rotated, keys, preferred_element_type=jnp.float32)
    scores = jnp.where(allowed[None], scores, masked_score)
    row_max = jnp.max(scores, axis=-1, keepdims=True)
    weights = jnp.exp(scores - row_max)
    probs = weights / jnp.sum(weights, axis=-1, keepdims=True)
    probs_low = probs.astype(jnp.bfloat16)
    attn_vals = (
        jnp.einsum("hts,sd->thd", probs_low, values, preferred_element_type=jnp.float32)
        .reshape(seq_len, heads_here * head_dim)
        .astype(jnp.bfloat16)
    )
    mid = inputs_f + lax.psum_scatter(
        matmul_nt(attn_vals, out_weight).astype(jnp.bfloat16),
        "mp",
        scatter_dimension=0,
        tiled=True,
    ).astype(jnp.float32)
    normed_two = norm_gain(mid, gain_two).astype(jnp.bfloat16)
    normed_all = lax.all_gather(normed_two, ("z", "mp"), axis=0, tiled=True)

    mixed_part, normed_part, weight_parts = ffn_pass(
        normed_all, grad_all, gate_weight, up_weight, down_weight
    )
    grad_normed_two = lax.psum_scatter(
        normed_part, ("z", "mp"), scatter_dimension=0, tiled=True
    ).astype(jnp.float32)
    mixed = (
        mid
        + lax.psum_scatter(mixed_part, ("z", "mp"), scatter_dimension=0, tiled=True).astype(
            jnp.float32
        )
    ).astype(jnp.bfloat16)

    def collect(part):
        pieces = part.reshape(z_size, xc_size, rows, unit).transpose(1, 0, 2, 3)
        pieces = pieces.reshape(xc_size * z_size * rows, unit)
        pieces = lax.psum_scatter(pieces, "xc", scatter_dimension=0, tiled=True)
        pieces = pieces.reshape(z_size, rows, unit)
        pieces = lax.all_to_all(pieces, "z", split_axis=0, concat_axis=0, tiled=True)
        return pieces.transpose(1, 0, 2).reshape(rows, z_size * unit).astype(jnp.float32)

    w_gate_grad, w_up_grad, w_down_grad = [collect(part) for part in weight_parts]

    norm_pull_two = jax.vjp(norm_gain, mid, gain_two)[1]
    grad_mid_norm, grad_gain_two = norm_pull_two(grad_normed_two)
    grad_mid = cotangent.astype(jnp.float32) + grad_mid_norm
    grad_mid_all = lax.all_gather(grad_mid.astype(jnp.bfloat16), "mp", axis=0, tiled=True)
    grad_vals = (
        jnp.dot(grad_mid_all, out_weight, preferred_element_type=jnp.float32)
        .astype(jnp.bfloat16)
        .reshape(seq_len, heads_here, head_dim)
    )
    grad_probs = jnp.einsum("thd,sd->hts", grad_vals, values, preferred_element_type=jnp.float32)
    delta = jnp.sum(probs * grad_probs, axis=-1, keepdims=True)
    grad_scores = (probs * (grad_probs - delta)).astype(jnp.bfloat16)
    grad_rot = jnp.einsum("hts,sd->thd", grad_scores, keys, preferred_element_type=jnp.float32)
    key_sum = jnp.einsum("hts,thd->sd", grad_scores, rotated, preferred_element_type=jnp.float32)
    value_sum = jnp.einsum("hts,thd->sd", probs_low, grad_vals, preferred_element_type=jnp.float32)
    grad_query = (
        (unrotate(grad_rot, cosine[:, None], sine[:, None]) * scale)
        .reshape(seq_len, heads_here * head_dim)
        .astype(jnp.bfloat16)
    )
    grad_kv = jnp.concatenate([unrotate(key_sum, cosine, sine), value_sum], axis=1).astype(
        jnp.bfloat16
    )
    grad_normed_one = lax.psum_scatter(
        (matmul_nt(grad_query, query_weight) + matmul_nt(grad_kv, kv_weight)).astype(jnp.bfloat16),
        "mp",
        scatter_dimension=0,
        tiled=True,
    ).astype(jnp.float32)
    norm_pull_one = jax.vjp(norm_gain, inputs_f, gain_one)[1]
    grad_input_norm, grad_gain_one = norm_pull_one(grad_normed_one)
    tokens_grad = (grad_mid + grad_input_norm).astype(jnp.bfloat16)

    w_query_grad = lax.psum_scatter(
        matmul_tn(normed_one, grad_query).astype(jnp.bfloat16), dp, scatter_dimension=0, tiled=True
    ).astype(jnp.float32)
    w_out_grad = lax.psum_scatter(
        matmul_tn(grad_mid_all, attn_vals).astype(jnp.bfloat16), dp, scatter_dimension=0, tiled=True
    ).astype(jnp.float32)
    small = jnp.concatenate(
        [matmul_tn(normed_one, grad_kv), grad_gain_one[:, None], grad_gain_two[:, None]], axis=1
    )
    small = lax.psum_scatter(small, everywhere, scatter_dimension=0, tiled=True)
    kv_grad = small[:, : 2 * head_dim]
    return (
        mixed,
        tokens_grad,
        small[:, 2 * head_dim],
        small[:, 2 * head_dim + 1],
        kv_grad,
        w_query_grad,
        w_out_grad,
        w_gate_grad,
        w_up_grad,
        w_down_grad,
    )


def shards_fast(
    tokens,
    segments,
    positions,
    cotangent,
    attn_gain,
    ffn_gain,
    w_kv,
    w_query,
    w_out,
    w_gate,
    w_up,
    w_down,
):
    quarter = w_kv.shape[1] // 8
    lane = jnp.arange(2 * quarter)
    freqs = rope_base ** (-(lane % quarter).astype(jnp.float32) / quarter)
    phase = positions.astype(jnp.float32)[:, None] * freqs[None, :]
    table = (jnp.cos(phase), jnp.where(lane < quarter, -1.0, 1.0)[None, :] * jnp.sin(phase))
    (
        normed_one,
        rotated,
        keys,
        values,
        attn_vals,
        mid,
        normed_two,
        gains,
        allowed,
        kv_weight,
        query_weight,
        out_weight,
        ffn_weights,
        grad_all,
    ) = pre_call(
        tokens,
        w_kv,
        attn_gain[None, :],
        ffn_gain[None, :],
        table,
        segments[None, :],
        cotangent,
        w_query,
        w_out,
        (w_gate, w_up, w_down),
    )
    main = ragged_split(w_gate.shape[1], lax.axis_size("z"))[0]
    grad_mid, gain_part, mix_parts, ffn_sums, grad_mid_low = ffn_call(
        gains, normed_two, grad_all, ffn_weights, mid, w_gate.shape[0], main
    )
    mixed, tokens_grad, gain_grads, kv_grad, query_grad, out_grad, ffn_grads = post_call(
        tokens,
        gains,
        gain_part,
        normed_one,
        rotated,
        keys,
        values,
        attn_vals,
        table,
        allowed,
        kv_weight,
        query_weight,
        out_weight,
        mix_parts,
        grad_mid,
        grad_mid_low,
        mid,
        ffn_sums,
        main,
    )
    *ffn_out, query_grad, out_grad, kv_grad, mixed, tokens_grad = layout_call(
        ffn_sums,
        ffn_grads,
        query_grad,
        out_grad,
        kv_grad,
        mixed,
        tokens_grad,
        w_gate.shape[1],
    )
    share = attn_gain.shape[0]
    place = lax.axis_index(("z", "x", "c", "mp")) * share
    gain_grads = gain_grads.reshape(2, gain_grads.size // 2)
    gain_grads = lax.dynamic_slice(gain_grads, (0, place), (2, share))
    return (
        mixed,
        tokens_grad,
        gain_grads[0],
        gain_grads[1],
        kv_grad,
        query_grad,
        out_grad,
        *ffn_out,
    )


def solution(mesh):
    dp_size, mp_size = mesh.shape["dp"], mesh.shape["mp"]
    if dp_size == 4 * FF_SPLIT and mp_size == 2:
        body, dp = shards_fast, ("z", "x", "c")
        sizes = (FF_SPLIT, 2, 2, mp_size)
    else:
        body, dp = shards_general, ("z", "xc")
        sizes = (FF_SPLIT, dp_size // FF_SPLIT, mp_size)
    all_axes = (*dp, "mp")
    fine = jax.sharding.Mesh(mesh.devices.reshape(sizes), all_axes)
    in_specs = (
        P(all_axes, None),
        P(dp),
        P(dp),
        P(all_axes, None),
        P(all_axes),
        P(all_axes),
        P(all_axes, None),
        P(dp, "mp"),
        P(dp, "mp"),
        P(dp, "mp"),
        P(dp, "mp"),
        P(dp, "mp"),
    )
    out_specs = (
        P(all_axes, None),
        P(all_axes, None),
        P(all_axes),
        P(all_axes),
        P(all_axes, None),
        P(dp, "mp"),
        P(dp, "mp"),
        P(dp, "mp"),
        P(dp, "mp"),
        P(dp, "mp"),
    )
    return jax.shard_map(body, mesh=fine, in_specs=in_specs, out_specs=out_specs, check_vma=False)
```

```python
import functools

import jax
import jax.numpy as jnp
from jax import lax
from jax.experimental import pallas as pl
from jax.experimental.pallas import tpu as pltpu
from jax.sharding import PartitionSpec as P

WINDOW = 2048


epsilon = 1e-06
rope_base = 10000.0
masked_score = -1e30
VMEM_BYTES = 66_000_000


def norm_gain(values, gain):
    return values * lax.rsqrt(jnp.mean(values * values, axis=-1, keepdims=True) + epsilon) * gain


def rotary_angles(positions, head_width):
    quarter = head_width // 4
    freqs = rope_base ** (-jnp.arange(quarter).astype(jnp.float32) / quarter)
    phase = positions.astype(jnp.float32)[:, None] * freqs[None, :]
    return (jnp.cos(phase), jnp.sin(phase))


def rotate(values, cosine, sine):
    quarter = cosine.shape[-1]
    first_half = values[..., :quarter]
    second_half = values[..., quarter : 2 * quarter]
    return jnp.concatenate(
        [
            first_half * cosine - second_half * sine,
            second_half * cosine + first_half * sine,
            values[..., 2 * quarter :],
        ],
        axis=-1,
    )


def unrotate(values, cosine, sine):
    quarter = cosine.shape[-1]
    first_half = values[..., :quarter]
    second_half = values[..., quarter : 2 * quarter]
    return jnp.concatenate(
        [
            first_half * cosine + second_half * sine,
            second_half * cosine - first_half * sine,
            values[..., 2 * quarter :],
        ],
        axis=-1,
    )


def gelu_product(gate, up_proj):
    return jax.nn.gelu(gate, approximate=True) * up_proj


def matmul_nt(left, right):
    return lax.dot_general(
        left, right, (((1,), (1,)), ((), ())), preferred_element_type=jnp.float32
    )


def matmul_tn(left, right):
    return lax.dot_general(
        left, right, (((0,), (0,)), ((), ())), preferred_element_type=jnp.float32
    )


def block_allowed(segments, first_row, rows):
    seq_len = segments.shape[0]
    query_rows = first_row + jnp.arange(rows)
    key_rows = jnp.arange(seq_len)
    return (
        (segments[:, None] == segments[None, :])
        & (key_rows[None, :] <= query_rows[:, None])
        & (query_rows[:, None] - key_rows[None, :] < WINDOW)
    )


MESH_ID = pl.DeviceIdType.MESH
GELU_A = 0.7978845608028654
GELU_B = 0.044715
TILE = 256
WIDE = 512


def remote(src, dst, send_sem, recv_sem, where):
    return pltpu.make_async_remote_copy(
        src_ref=src,
        dst_ref=dst,
        send_sem=send_sem,
        recv_sem=recv_sem,
        device_id=where,
        device_id_type=MESH_ID,
    )


class Halves:
    def __init__(self, src, dst, send_sem, recv_sem, where):
        rows = src.shape[0] // 2
        cuts = [pl.ds(part * rows, rows) for part in range(2)]
        self.copies = [
            remote(src.at[cut], dst.at[cut], send_sem.at[part], recv_sem.at[part], where)
            for part, cut in enumerate(cuts)
        ]

    def start(self):
        for copy in self.copies:
            copy.start()

    def wait_recv(self):
        for copy in self.copies:
            copy.wait_recv()

    def wait_send(self):
        for copy in self.copies:
            copy.wait_send()


def dot_nn(left, right):
    return lax.dot_general(
        left, right, (((1,), (0,)), ((), ())), preferred_element_type=jnp.float32
    )


def gelu_parts(gate):
    square = gate * gate
    bend = jnp.tanh(GELU_A * gate * (1.0 + GELU_B * square))
    half = 0.5 * (1.0 + bend)
    slope = half + 0.5 * gate * (1.0 - bend * bend) * GELU_A * (1.0 + 3.0 * GELU_B * square)
    return gate * half, slope


def add_rows(first, rest, out, count):
    def body(index, carry):
        step = pl.ds(pl.multiple_of(index * 32, 32), 32)
        total = first[step, :].astype(jnp.float32)
        for other in rest:
            total = total + other[step, :].astype(jnp.float32)
        out[step, :] = total.astype(out.dtype)
        return carry

    lax.fori_loop(0, count // 32, body, 0)


def norm_back(values, gain, upstream):
    scale = lax.rsqrt(jnp.mean(values * values, axis=-1, keepdims=True) + epsilon)
    normed = values * scale
    pulled = gain * upstream
    back = scale * (pulled - normed * jnp.mean(normed * pulled, axis=-1, keepdims=True))
    return back, jnp.sum(upstream * normed, axis=0, keepdims=True)


def ffn_kernel(
    z_size,
    main,
    gain_ref,
    own_hbm,
    dy_hbm,
    w_hbm,
    mid_hbm,
    gm_ref,
    gain_part,
    mix_hbm,
    sums_hbm,
    gm_hbm,
    n2,
    dy,
    w3,
    h3,
    n2_t,
    dy_t,
    gn_part,
    mix_buf,
    gn_y,
    gn_z,
    gn_s,
    c_in,
    x_in,
    mid,
    load_sem,
    mix_sem,
    ag_y_send,
    ag_y_recv,
    ag_z_send,
    ag_z_recv,
    rs_y_send,
    rs_y_recv,
    rs_z_send,
    rs_z_recv,
    c_send,
    c_recv,
    x_send,
    x_recv,
    out_sem,
):
    own = own_hbm.shape[0] // 2
    width = own_hbm.shape[1]
    units = w3.shape[2]
    rows = c_in.shape[3]
    span = width // z_size
    me_y, me_z = lax.axis_index("mp"), lax.axis_index("z")
    me_x, me_c = lax.axis_index("x"), lax.axis_index("c")
    mine = pl.ds(pl.multiple_of(me_y * own, own), own)
    theirs = pl.ds(pl.multiple_of((1 - me_y) * own, own), own)
    to_y, to_x, to_c = {"mp": 1 - me_y}, {"x": 1 - me_x}, {"c": 1 - me_c}

    def ahead(step):
        return lax.rem(me_z + step, z_size)

    def to_z(step):
        return {"z": ahead(step)}

    def row_block(z_at, x_at, c_at):
        return pl.ds(pl.multiple_of(((z_at * 2 + x_at) * 2 + c_at) * rows, rows), rows)

    inner = (me_z > 0) & (me_z < z_size - 1)
    outer = (me_z == 0) | (me_z == z_size - 1)

    def w_load(index, columns):
        cols = pl.ds(0, columns)
        return pltpu.make_async_copy(
            w_hbm.at[index, :, cols], w3.at[index, :, cols], load_sem.at[z_size + index]
        )

    def w_loads(act):
        for case, columns in ((inner, units), (outer, main)):

            @pl.when(case)
            def _(columns=columns):
                for index in range(3):
                    act(w_load(index, columns))

    w_loads(lambda copy: copy.start())
    dy_loads = [
        pltpu.make_async_copy(dy_hbm.at[index], dy, load_sem.at[index])
        for index in range(z_size)
    ]
    own_load = pltpu.make_async_copy(own_hbm, n2.at[0], load_sem.at[z_size + 3])
    mid_load = pltpu.make_async_copy(mid_hbm, mid, load_sem.at[z_size + 4])
    for load in (own_load, dy_loads[0], mid_load):
        load.start()

    barrier = pltpu.get_barrier_semaphore()
    peers = [to_y, to_x, to_c] + [to_z(step) for step in range(1, z_size)]
    for where in peers:
        pl.semaphore_signal(barrier, inc=1, device_id=where, device_id_type=MESH_ID)
    pl.semaphore_wait(barrier, len(peers))

    def ag_y(index):
        block = n2.at[index, mine]
        return Halves(block, block, ag_y_send.at[index], ag_y_recv.at[index], to_y)

    def ag_y_in(index):
        block = n2.at[index, theirs]
        return Halves(block, block, ag_y_send.at[index], ag_y_recv.at[index], to_y)

    def ag_z(index):
        src = own_hbm.at[mine] if index == 0 else n2.at[index, mine]
        return Halves(
            src, n2.at[index + 1, mine], ag_z_send.at[index], ag_z_recv.at[index + 1], to_z(1)
        )

    def ag_z_in(index):
        block = n2.at[index, mine]
        return Halves(block, block, ag_z_send.at[0], ag_z_recv.at[index], to_z(1))

    def ag_last():
        return Halves(
            n2.at[2, theirs], n2.at[3, theirs], ag_y_send.at[3], ag_y_recv.at[3], to_z(1)
        )

    def forward(index):
        ag_z_in(index).wait_recv()
        ag_z(index).start()
        ag_y(index).start()

    ag_z(0).start()

    mix_copies = []

    def turn(source, target, index):
        def turn_tile(tile, carry):
            at = pl.ds(pl.multiple_of(tile * span, 128), span)
            target[at, pl.ds(index * 2 * own, 2 * own)] = source[:, at].T
            return carry

        lax.fori_loop(0, z_size, turn_tile, 0)

    def chunk(index):
        if index:
            mix_copies[index - 1].wait()
        dy_loads[index].wait()
        rows_at = pl.ds(index * 2 * own, 2 * own)

        def up_tile(tile, carry):
            cols = pl.ds(pl.multiple_of(tile * WIDE, WIDE), WIDE)
            gate = dot_nn(n2[index], w3[0, :, cols])
            up_proj = dot_nn(n2[index], w3[1, :, cols])
            grad_hidden = dot_nn(dy[...], w3[2, :, cols])
            act, slope = gelu_parts(gate)
            h3[0, rows_at, cols] = (grad_hidden * up_proj * slope).astype(jnp.bfloat16)
            h3[1, rows_at, cols] = (grad_hidden * act).astype(jnp.bfloat16)
            h3[2, rows_at, cols] = (act * up_proj).astype(jnp.bfloat16)
            return carry

        lax.fori_loop(0, units // WIDE, up_tile, 0)

        def down_tile(tile, carry):
            at = pl.ds(pl.multiple_of(tile * span, 128), span)
            normed = matmul_nt(w3[0, at, :], h3[0, rows_at, :]) + matmul_nt(
                w3[1, at, :], h3[1, rows_at, :]
            )
            mixed = matmul_nt(w3[2, at, :], h3[2, rows_at, :])
            for half in range(2):
                cols = slice(half * own, (half + 1) * own)
                gn_part[index, half, at, :] = normed[:, cols].astype(jnp.bfloat16)
                mix_buf[half, at, :] = mixed[:, cols].astype(jnp.bfloat16)
            return carry

        lax.fori_loop(0, z_size, down_tile, 0)
        copy = pltpu.make_async_copy(mix_buf, mix_hbm.at[index], mix_sem.at[index])
        copy.start()
        mix_copies.append(copy)
        if index:
            rs_y(index).start()
        turn(n2.at[index], n2_t, index)
        turn(dy, dy_t, index)
        if index + 1 < z_size:
            dy_loads[index + 1].start()

    def rs_y(index):
        return Halves(
            gn_part.at[index, 1 - me_y], gn_y.at[index], rs_y_send.at[index], rs_y_recv.at[index], to_y
        )

    def rs_z(index):
        return Halves(
            gn_s.at[index - 1],
            gn_z.at[index - 1],
            rs_z_send.at[index],
            rs_z_recv.at[index - 1],
            to_z(1),
        )

    def rs_step(index):
        rs_y(index).wait_recv()
        slot = (index - 2) % z_size
        if index != 1:
            Halves(
                gn_s.at[slot], gn_z.at[slot], rs_z_send.at[1], rs_z_recv.at[slot], to_z(1)
            ).wait_recv()

        def add_tile(tile, carry):
            at = pl.ds(pl.multiple_of(tile * TILE, TILE), TILE)
            total = gn_part[index, me_y, at, :].astype(jnp.float32) + gn_y[index, at, :].astype(
                jnp.float32
            )
            if index != 1:
                total = total + gn_z[slot, at, :].astype(jnp.float32)
            if index == 0:
                gm_ref[:, at] = total.T
            else:
                gn_s[index - 1, at, :] = total.astype(jnp.bfloat16)
            return carry

        lax.fori_loop(0, width // TILE, add_tile, 0)
        if index != 0:
            rs_z(index).start()


    def grads(step):
        at = pl.ds(pl.multiple_of(ahead(step) * span, 128), span)
        for kind, source in enumerate((n2_t, n2_t, dy_t)):

            def tile_body(tile, carry, kind=kind, source=source):
                cols = pl.ds(pl.multiple_of(tile * WIDE, WIDE), WIDE)
                w3[kind, at, cols] = dot_nn(source[at, :], h3[kind, :, cols]).astype(jnp.bfloat16)
                return carry

            lax.fori_loop(0, units // WIDE, tile_body, 0)
            for far in (1, 0):
                over_c(kind, step, far).start()

    def over_c(kind, step, far):
        x_at = 1 - me_x if far else me_x
        return remote(
            w3.at[kind, row_block(ahead(step), x_at, 1 - me_c)],
            c_in.at[kind, step, far],
            c_send.at[kind, step, far],
            c_recv.at[kind, step, far],
            to_c,
        )

    def over_x(kind):
        return remote(
            w3.at[kind, row_block(ahead(1), 1 - me_x, me_c)],
            x_in.at[kind],
            x_send.at[kind],
            x_recv.at[kind],
            to_x,
        )

    out_copies = []

    def keep(kind, step, far, block):
        copy = pltpu.make_async_copy(
            block, sums_hbm.at[kind, step, far], out_sem.at[kind, step, far]
        )
        copy.start()
        out_copies.append(copy)

    def core_sums(step):
        pairs = [(kind, far) for kind in range(3) for far in (1, 0)]
        if step == 1:
            pairs.sort(key=lambda pair: -pair[1])
        for kind, far in pairs:
            over_c(kind, step, far).wait_recv()
            x_at = 1 - me_x if far else me_x
            block = w3.at[kind, row_block(ahead(step), x_at, me_c)]
            add_rows(block, [c_in.at[kind, step, far]], block, rows)
            if step != 1:
                keep(kind, step, far, block)
            elif far:
                over_x(kind).start()

    def first_sums():
        for kind in range(3):
            over_x(kind).wait_recv()
            block = w3.at[kind, row_block(ahead(1), me_x, me_c)]
            add_rows(block, [x_in.at[kind]], block, rows)
            keep(kind, 1, 0, block)

    own_load.wait()
    w_loads(lambda copy: copy.wait())

    @pl.when(outer)
    def _():
        w3[:, :, main:] = jnp.zeros((3, width, units - main), jnp.bfloat16)

    chunk(0)
    forward(1)
    forward(2)
    ag_y_in(1).wait_recv()
    chunk(1)
    ag_y_in(2).wait_recv()
    ag_last().start()
    chunk(2)
    rs_step(1)
    ag_z_in(3).wait_recv()
    ag_last().wait_recv()
    chunk(3)
    rs_y(0).start()
    rs_step(2)
    grads(1)
    grads(2)
    core_sums(1)
    rs_step(3)
    grads(3)
    core_sums(2)
    grads(0)
    core_sums(3)
    rs_step(0)
    core_sums(0)

    cot_load = pltpu.make_async_copy(
        dy_hbm.at[0, mine], dy.at[pl.ds(0, own)], load_sem.at[z_size + 3]
    )
    cot_load.start()
    cot_load.wait()
    mid_load.wait()

    def mid_rows(index, total):
        at = pl.ds(pl.multiple_of(index * 32, 32), 32)
        grad, gain_sum = norm_back(mid[at, :], gain_ref[1:2, :], gm_ref[at, :])
        grad = grad + dy[at, :].astype(jnp.float32)
        gm_ref[at, :] = grad
        dy[pl.ds(pl.multiple_of(own + index * 32, 32), 32), :] = grad.astype(jnp.bfloat16)
        return total + gain_sum

    gain_sum = lax.fori_loop(0, own // 32, mid_rows, jnp.zeros((1, width), jnp.float32))
    gm_save = pltpu.make_async_copy(dy.at[pl.ds(own, own)], gm_hbm, load_sem.at[z_size + 3])
    gm_save.start()
    for index in range(4):
        gain_part[index : index + 1, :] = jnp.zeros((1, span), jnp.float32)
        gain_part[4 + index : 5 + index, :] = gain_sum[:, index * span : (index + 1) * span]
    first_sums()
    gm_save.wait()

    for copy in mix_copies[3:] + out_copies:
        copy.wait()
    for index in range(z_size):
        if index in (1, 2):
            ag_y(index).wait_send()
        if index == 3:
            ag_last().wait_send()
        rs_y(index).wait_send()
        if index < z_size - 1:
            ag_z(index).wait_send()
        if index:
            rs_z(index).wait_send()
        for kind in range(3):
            over_c(kind, index, 0).wait_send()
            over_c(kind, index, 1).wait_send()
            if index == 1:
                over_x(kind).wait_send()


def ffn_call(gains, normed, grad_all, weights, mid, rows, main):
    z_size = lax.axis_size("z")
    pair, width = normed.shape
    units = weights.shape[2]
    own = pair // 2
    wide = lambda *lead: pltpu.VMEM((*lead, width), jnp.bfloat16)
    tall = lambda *lead: pltpu.VMEM((*lead, width, own), jnp.bfloat16)
    dma = lambda *lead: pltpu.SemaphoreType.DMA(lead)
    vmem = pl.BlockSpec(memory_space=pltpu.VMEM)
    hbm = pl.BlockSpec(memory_space=pl.ANY)
    return pl.pallas_call(
        functools.partial(ffn_kernel, z_size, main),
        out_shape=(
            jax.ShapeDtypeStruct((own, width), jnp.float32),
            jax.ShapeDtypeStruct((8, width // z_size), jnp.float32),
            jax.ShapeDtypeStruct((z_size, 2, width, own), jnp.bfloat16),
            jax.ShapeDtypeStruct((3, z_size, 2, rows, units), jnp.bfloat16),
            jax.ShapeDtypeStruct((own, width), jnp.bfloat16),
        ),
        in_specs=[vmem, hbm, hbm, hbm, hbm],
        out_specs=(vmem, vmem, hbm, hbm, hbm),
        scratch_shapes=[
            wide(z_size, pair),
            wide(pair),
            pltpu.VMEM(weights.shape, jnp.bfloat16),
            pltpu.VMEM((3, z_size * pair, units), jnp.bfloat16),
            pltpu.VMEM((width, z_size * pair), jnp.bfloat16),
            pltpu.VMEM((width, z_size * pair), jnp.bfloat16),
            tall(z_size, 2),
            tall(2),
            tall(z_size),
            tall(z_size - 1),
            tall(z_size - 1),
            pltpu.VMEM((3, z_size, 2, rows, units), jnp.bfloat16),
            pltpu.VMEM((3, rows, units), jnp.bfloat16),
            pltpu.VMEM((own, width), jnp.float32),
            dma(z_size + 5),
            dma(z_size),
            dma(z_size, 2),
            dma(z_size, 2),
            dma(z_size, 2),
            dma(z_size, 2),
            dma(z_size, 2),
            dma(z_size, 2),
            dma(z_size, 2),
            dma(z_size, 2),
            dma(3, z_size, 2),
            dma(3, z_size, 2),
            dma(3),
            dma(3),
            dma(3, z_size, 2),
        ],
        compiler_params=pltpu.CompilerParams(
            collective_id=0, has_side_effects=True, vmem_limit_bytes=VMEM_BYTES
        ),
        cost_estimate=pl.CostEstimate(
            flops=18 * z_size * pair * width * units,
            bytes_accessed=4 * weights.size + 12 * z_size * pair * width,
            transcendentals=z_size * pair * units,
        ),
    )(gains, normed, grad_all, weights, mid)


def spin(values, table):
    first = values[:, : values.shape[1] // 2]
    turned = first * table[0] + pltpu.roll(first, first.shape[1] // 2, 1) * table[1]
    return jnp.concatenate([turned, values[:, values.shape[1] // 2 :]], axis=1)


def spin_back(values, table):
    first = values[:, : values.shape[1] // 2]
    turned = first * table[0] - pltpu.roll(first, first.shape[1] // 2, 1) * table[1]
    return jnp.concatenate([turned, values[:, values.shape[1] // 2 :]], axis=1)


def head_probs(rotated, keys, allowed):
    scores = jnp.where(allowed > 0.5, matmul_nt(rotated, keys), masked_score)
    weights = jnp.exp(scores - jnp.max(scores, axis=-1, keepdims=True))
    return weights / jnp.sum(weights, axis=-1, keepdims=True)


def ragged_split(columns, parts):
    main = columns // parts // 128 * 128
    return main, main + 128


def pre_kernel(
    z_size,
    tok_ref,
    wkv_ref,
    gain_one_ref,
    gain_two_ref,
    cos_ref,
    sin_ref,
    seg_ref,
    cot_hbm,
    wq_hbm,
    wo_hbm,
    wg_hbm,
    wu_hbm,
    wd_hbm,
    n1_ref,
    rot_ref,
    key_ref,
    val_ref,
    att_ref,
    mid_ref,
    n2_ref,
    gain_ref,
    allow_ref,
    kv_out,
    wq_out,
    wo_out,
    w3_out,
    dy_out,
    kv_w,
    q_w,
    o_w,
    tok,
    part,
    part_y,
    query,
    gain_rows,
    y_send,
    y_recv,
    ky_send,
    ky_recv,
    az_send,
    az_recv,
    ax_send,
    ax_recv,
    ac_send,
    ac_recv,
    fz_send,
    fz_recv,
    fx_send,
    fx_recv,
    fc_send,
    fc_recv,
    dz_send,
    dz_recv,
    dy_send,
    dy_recv,
    local_sem,
):
    me_z, me_x = lax.axis_index("z"), lax.axis_index("x")
    me_c, me_y = lax.axis_index("c"), lax.axis_index("mp")
    own, width = tok_ref.shape
    rows = wq_hbm.shape[0]
    half_rows = wkv_ref.shape[0]
    head = key_ref.shape[1]
    main, units = ragged_split(wg_hbm.shape[1], z_size)
    to_y, to_x, to_c = {"mp": 1 - me_y}, {"x": 1 - me_x}, {"c": 1 - me_c}

    def to_z(step):
        return {"z": lax.rem(me_z + step, z_size)}

    def from_z(step):
        return lax.rem(me_z - step + z_size, z_size)

    def row_block(step, x_at, c_at):
        start = ((from_z(step) * 2 + x_at) * 2 + c_at) * rows
        return pl.ds(pl.multiple_of(start, rows), rows)

    mine = pl.ds(pl.multiple_of(me_y * own, own), own)
    theirs = pl.ds(pl.multiple_of((1 - me_y) * own, own), own)
    bufs = (kv_w, q_w, o_w)
    inputs = (None, wq_hbm, wo_hbm)

    locals_ = []

    def local(src, dst):
        copy = pltpu.make_async_copy(src, dst, local_sem.at[len(locals_)])
        copy.start()
        locals_.append(copy)
        return copy

    here = row_block(0, me_x, me_c)
    own_q = local(wq_hbm, q_w.at[here])
    own_o = local(wo_hbm, o_w.at[here])
    ffn_in = (wg_hbm, wu_hbm, wd_hbm)

    def body_of(target):
        return pl.ds(pl.multiple_of(target * main, 128), main), pl.ds(0, main)

    def tail_of(target):
        start = z_size * main + lax.rem(target + 1, 2) * 128
        return pl.ds(pl.multiple_of(start, 128), 128), pl.ds(main, 128)

    def is_inner(at):
        return (at > 0) & (at < z_size - 1)

    own_f = []
    for kind in range(3):
        src, dst = body_of(me_z)
        own_f.append(local(ffn_in[kind].at[:, src], w3_out.at[kind, here, dst]))

    def own_tail(kind):
        src, dst = tail_of(me_z)
        return pltpu.make_async_copy(
            ffn_in[kind].at[:, src], w3_out.at[kind, here, dst], local_sem.at[12 + kind]
        )

    @pl.when(is_inner(me_z))
    def _():
        for kind in range(3):
            own_tail(kind).start()
    own_d = local(cot_hbm, dy_out.at[0, mine])

    kv_own = pl.ds(pl.multiple_of(here.start + me_y * half_rows, half_rows), half_rows)
    gain_rows[...] = jnp.zeros(gain_rows.shape, jnp.float32)
    gain_rows[0:1, :half_rows] = gain_one_ref[...].astype(jnp.float32)
    gain_rows[1:2, :half_rows] = gain_two_ref[...].astype(jnp.float32)
    spread = gain_rows[...].T
    kv_w[kv_own, : 2 * head] = wkv_ref[...]
    kv_w[kv_own, 2 * head :] = spread[:half_rows, :].astype(jnp.bfloat16)

    barrier = pltpu.get_barrier_semaphore()
    peers = [to_y, to_x, to_c] + [to_z(step) for step in range(1, z_size)]
    for where in peers:
        pl.semaphore_signal(barrier, inc=1, device_id=where, device_id_type=MESH_ID)
    pl.semaphore_wait(barrier, len(peers))

    tok_y = remote(tok_ref, tok.at[mine], y_send.at[1], y_recv.at[1], to_y)
    tok_y_in = remote(tok_ref, tok.at[theirs], y_send.at[1], y_recv.at[1], to_y)
    part_out = remote(part.at[theirs], part_y, y_send.at[2], y_recv.at[2], to_y)
    n2_y = remote(n2_ref.at[mine], n2_ref.at[mine], y_send.at[3], y_recv.at[3], to_y)
    n2_y_in = remote(n2_ref.at[theirs], n2_ref.at[theirs], y_send.at[3], y_recv.at[3], to_y)

    def block_of(kind, step, x_at):
        if kind:
            return row_block(step, x_at, me_c)
        return kv_rows(step, x_at, me_y)

    def kv_rows(step, x_at, y_at):
        start = row_block(step, x_at, me_c).start + y_at * half_rows
        return pl.ds(pl.multiple_of(start, half_rows), half_rows)

    def kv_y(step, far):
        x_at = 1 - me_x if far else me_x
        block = kv_w.at[kv_rows(step, x_at, me_y)]
        slot = step + z_size * far
        return remote(block, block, ky_send.at[slot], ky_recv.at[slot], to_y)

    def kv_y_in(step, far):
        x_at = 1 - me_x if far else me_x
        block = kv_w.at[kv_rows(step, x_at, 1 - me_y)]
        slot = step + z_size * far
        return remote(block, block, ky_send.at[slot], ky_recv.at[slot], to_y)

    def source(kind, step):
        if isinstance(step, int) and step == 0 and kind:
            return inputs[kind]
        return bufs[kind].at[block_of(kind, step, me_x)]

    first_z, last_z = (z_size - 1 - me_z) // (z_size - 1), me_z // (z_size - 1)
    inner = first_z + last_z == 0
    order = (0, 1 + 2 * first_z, 3 - first_z - last_z, 2 - first_z + last_z)
    hops = (
        None,
        (lax.rem(me_z + 1, z_size), 2),
        (lax.rem(me_z + z_size - 1, z_size), 2),
        (lax.rem(3 * (me_z + 3), z_size), lax.rem(2 * me_z + 3, z_size)),
    )

    def a_z_own(kind, right):
        return remote(
            source(kind, 0),
            bufs[kind].at[block_of(kind, 0, me_x)],
            az_send.at[kind, right],
            az_recv.at[kind, 1 if right else z_size - 1],
            to_z(1 if right else z_size - 1),
        )

    def a_z_start(kind):
        @pl.when(last_z == 0)
        def _():
            a_z_own(kind, 1).start()

        @pl.when(first_z == 0)
        def _():
            a_z_own(kind, 0).start()

    def a_z(kind, index):
        target, slot = hops[index]
        block = bufs[kind].at[block_of(kind, order[index], me_x)]
        return remote(
            block, block, az_send.at[kind, 1 + index], az_recv.at[kind, slot], {"z": target}
        )

    def a_z_next(kind, index):
        @pl.when(inner)
        def _():
            a_z(kind, index).start()

    def a_z_done(kind):
        @pl.when(last_z == 0)
        def _():
            a_z_own(kind, 1).wait_send()

        @pl.when(first_z == 0)
        def _():
            a_z_own(kind, 0).wait_send()

        @pl.when(inner)
        def _():
            for index in range(1, z_size):
                a_z(kind, index).wait_send()

    def a_z_in(kind, step):
        block = bufs[kind].at[block_of(kind, step, me_x)]
        return remote(block, block, az_send.at[kind, 0], az_recv.at[kind, step], to_z(1))

    def a_x(kind, step):
        return remote(
            source(kind, step),
            bufs[kind].at[block_of(kind, step, me_x)],
            ax_send.at[kind, step],
            ax_recv.at[kind, step],
            to_x,
        )

    def a_x_in(kind, step):
        block = bufs[kind].at[block_of(kind, step, 1 - me_x)]
        return remote(block, block, ax_send.at[kind, step], ax_recv.at[kind, step], to_x)

    def a_c(kind, step, far):
        x_at = 1 - me_x if far else me_x
        block = bufs[kind].at[row_block(step, x_at, me_c)]
        src = source(kind, step) if kind and not far else block
        slot = step + z_size * far
        return remote(src, block, ac_send.at[kind, slot], ac_recv.at[kind, slot], to_c)

    def a_c_in(kind, step, far):
        x_at = 1 - me_x if far else me_x
        block = bufs[kind].at[row_block(step, x_at, 1 - me_c)]
        slot = step + z_size * far
        return remote(block, block, ac_send.at[kind, slot], ac_recv.at[kind, slot], to_c)

    def f_z(kind, step, act):
        target = lax.rem(me_z + step, z_size)

        def piece(index, src, dst):
            return remote(
                ffn_in[kind].at[:, src],
                w3_out.at[kind, here, dst],
                fz_send.at[kind, step, index],
                fz_recv.at[kind, step, index],
                to_z(step),
            )

        act(piece(0, *body_of(target)))

        @pl.when(is_inner(target))
        def _():
            act(piece(1, *tail_of(target)))

    def f_z_wait(kind, step):
        block = row_block(step, me_x, me_c)

        def piece(index, dst):
            part = w3_out.at[kind, block, dst]
            return remote(
                part, part, fz_send.at[kind, step, index], fz_recv.at[kind, step, index], to_z(step)
            )

        piece(0, pl.ds(0, main)).wait_recv()

        @pl.when(inner)
        def _():
            piece(1, pl.ds(main, 128)).wait_recv()

    def f_x(kind, step, x_at, act):
        for case, columns in ((inner, units), (first_z + last_z > 0, main)):

            @pl.when(case)
            def _(columns=columns):
                block = w3_out.at[kind, row_block(step, x_at, me_c), pl.ds(0, columns)]
                act(remote(block, block, fx_send.at[kind, step], fx_recv.at[kind, step], to_x))

    def f_x_start(kind, step):
        f_x(kind, step, me_x, lambda copy: copy.start())

    def f_x_wait(kind, step):
        f_x(kind, step, 1 - me_x, lambda copy: copy.wait_recv())

    def f_x_done(kind, step):
        f_x(kind, step, me_x, lambda copy: copy.wait_send())

    def f_c(kind, step, far):
        block = w3_out.at[kind, row_block(step, 1 - me_x if far else me_x, me_c)]
        slot = step + z_size * far
        return remote(block, block, fc_send.at[kind, slot], fc_recv.at[kind, slot], to_c)

    def f_c_in(kind, step, far):
        block = w3_out.at[kind, row_block(step, 1 - me_x if far else me_x, 1 - me_c)]
        slot = step + z_size * far
        return remote(block, block, fc_send.at[kind, slot], fc_recv.at[kind, slot], to_c)

    def d_source(step):
        return cot_hbm if isinstance(step, int) else dy_out.at[step, mine]

    def d_z_own(right):
        slot = 1 if right else z_size - 1
        return remote(
            cot_hbm, dy_out.at[slot, mine], dz_send.at[right], dz_recv.at[slot], to_z(slot)
        )

    def d_z(index):
        target, slot = hops[index]
        return remote(
            dy_out.at[order[index], mine],
            dy_out.at[slot, mine],
            dz_send.at[1 + index],
            dz_recv.at[slot],
            {"z": target},
        )

    def d_z_done():
        @pl.when(last_z == 0)
        def _():
            d_z_own(1).wait_send()

        @pl.when(first_z == 0)
        def _():
            d_z_own(0).wait_send()

        @pl.when(inner)
        def _():
            for index in range(1, z_size):
                d_z(index).wait_send()

    def d_z_in(step):
        block = dy_out.at[step, mine]
        return remote(block, block, dz_send.at[0], dz_recv.at[step], to_z(1))

    def d_y(step):
        return remote(
            d_source(step), dy_out.at[step, mine], dy_send.at[step], dy_recv.at[step], to_y
        )

    def d_y_in(step):
        block = dy_out.at[step, theirs]
        return remote(block, block, dy_send.at[step], dy_recv.at[step], to_y)

    for kind in (1, 0, 2):
        a_z_start(kind)
        a_x(kind, 0).start()
    kv_y(0, 0).start()
    tok_y.start()
    for kind in (1, 2):
        a_c(kind, 0, 0).start()

    for at_end, away in ((first_z, 1), (last_z, z_size - 1)):

        @pl.when(at_end > 0)
        def _(away=away):
            d_z_own(1 if away == 1 else 0).start()
            for kind in range(3):
                f_z(kind, away, lambda copy: copy.start())

    tok[mine, :] = tok_ref[...]
    seq = 2 * own
    query_at = lax.broadcasted_iota(jnp.int32, (seq, seq), 0)
    key_at = lax.broadcasted_iota(jnp.int32, (seq, seq), 1)
    segment = seg_ref[...].astype(jnp.float32)
    same = jnp.broadcast_to(segment, (8, seq)).T[:, :1] == segment
    allowed = same & (key_at <= query_at) & (query_at - key_at < WINDOW)
    allow_ref[...] = jnp.where(allowed, 1.0, 0.0)
    d_y(0).start()

    def pass_cotangent(index):
        d_z_in(order[index]).wait_recv()

        @pl.when(inner)
        def _():
            d_z(index).start()

        d_y(order[index]).start()

    def pass_at(at, index):
        @pl.when(me_z == at)
        def _():
            pass_cotangent(index)

    def pass_if(case, index):
        @pl.when(case)
        def _():
            pass_cotangent(index)

    outer = first_z + last_z > 0

    def from_x(index):
        step = order[index]
        for kind in (1, 0, 2):
            a_x_in(kind, step).wait_recv()
            if kind:
                a_c(kind, step, 1).start()
            else:
                kv_y(step, 1).start()

    def from_y(index):
        step = order[index]
        for far in range(2):
            kv_y_in(step, far).wait_recv()
            a_c(0, step, far).start()

    for index in range(1, z_size):
        step = order[index]
        for kind in (1, 0, 2):
            a_z_in(kind, step).wait_recv()
            a_z_next(kind, index)
            a_x(kind, step).start()
            if kind:
                a_c(kind, step, 0).start()
            else:
                kv_y(step, 0).start()
        if index == z_size - 2:

            @pl.when(inner)
            def _():
                d_z_own(1).start()
                d_z_own(0).start()

        if index == z_size - 1:
            pass_at(1, 1)
            pass_at(2, 2)
            for copy in own_f:
                copy.wait()

            @pl.when(inner)
            def _():
                for kind in range(3):
                    own_tail(kind).wait()

            for case, ways in ((inner, (2, 1, 3)), (first_z > 0, (3, 2)), (last_z > 0, (1, 2))):

                @pl.when(case)
                def _(ways=ways):
                    for away in ways:
                        for kind in range(3):
                            f_z(kind, away, lambda copy: copy.start())

            for kind in range(3):
                f_x_start(kind, 0)
                f_c(kind, 0, 0).start()
        if index >= 2:
            from_x(index - 2)
            from_y(index - 2)
    from_x(z_size - 2)
    from_y(z_size - 2)
    pass_at(1, 2)
    pass_at(2, 1)
    pass_if(outer, 1)
    from_x(z_size - 1)
    from_y(z_size - 1)

    def hand_on(kind, step):
        f_z_wait(kind, step)
        f_x_start(kind, step)
        f_c(kind, step, 0).start()

    def hand_if(case, *blocks):
        @pl.when(case)
        def _():
            for kind, index in blocks:
                hand_on(kind, order[index])

    def cross(kind, step):
        f_x_wait(kind, step)
        f_c(kind, step, 1).start()

    tok_y_in.wait_recv()
    own_q.wait()
    own_o.wait()
    for kind in (0, 1):
        for step in range(z_size):
            for far in range(2):
                a_c_in(kind, step, far).wait_recv()

    gains = kv_w[:, 2 * head :].astype(jnp.float32).T[:8, :]
    gain_ref[...] = gains

    def norm_rows(index, carry):
        at = pl.ds(pl.multiple_of(index * 32, 32), 32)
        values = tok[at, :].astype(jnp.float32)
        scale = lax.rsqrt(jnp.mean(values * values, axis=-1, keepdims=True) + epsilon)
        n1_ref[at, :] = (values * scale * gain_ref[0:1, :]).astype(jnp.bfloat16)
        return carry

    lax.fori_loop(0, 2 * own // 32, norm_rows, 0)
    pass_if(inner, 3)
    hand_if(inner, (0, 1), (1, 1))
    table = (cos_ref[...], sin_ref[...])
    key_ref[...] = spin(dot_nn(n1_ref[...], kv_w[:, :head]), table).astype(jnp.bfloat16)
    val_ref[...] = dot_nn(n1_ref[...], kv_w[:, head : 2 * head]).astype(jnp.bfloat16)
    head_scale = head ** (-0.5)
    heads = att_ref.shape[1] // head

    half_cols = att_ref.shape[1] // 2
    for index in range(2):
        cols = pl.ds(index * half_cols, half_cols)
        query[:, cols] = dot_nn(n1_ref[...], q_w[:, cols])

    def attend(index):
        cols = pl.ds(index * head, head)
        rotated = (spin(query[:, cols], table) * head_scale).astype(jnp.bfloat16)
        rot_ref[:, cols] = rotated
        probs = head_probs(rotated, key_ref[...], allow_ref[...]).astype(jnp.bfloat16)
        att_ref[:, cols] = dot_nn(probs, val_ref[...]).astype(jnp.bfloat16)

    tasks = [
        lambda: (hand_if(inner, (2, 1)), hand_if(outer, (0, 2))),
        lambda: cross(0, 0),
        lambda: (hand_if(inner, (0, 2)), hand_if(outer, (1, 2))),
        lambda: cross(1, 0),
        lambda: (hand_if(inner, (1, 2)), hand_if(outer, (2, 2)), cross(2, 0)),
    ]
    for index in range(heads):
        attend(index)
        if index < len(tasks):
            tasks[index]()
    for step in range(z_size):
        for far in range(2):
            a_c_in(2, step, far).wait_recv()
    saves = [
        local(kv_w, kv_out),
        local(q_w, wq_out),
        local(o_w, wo_out),
    ]
    span = width // 4

    def project(index, carry):
        cols = pl.ds(pl.multiple_of(index * span, span), span)
        part[:, cols] = matmul_nt(att_ref[...], o_w[cols, :]).astype(jnp.bfloat16)
        return carry

    lax.fori_loop(0, 4, project, 0)
    part_out.start()
    hand_if(inner, (2, 2))
    hand_if(outer, (0, 1), (0, 3))
    pass_if(outer, 2)
    part_out.wait_recv()

    def middle(index, carry):
        at = pl.ds(pl.multiple_of(index * 32, 32), 32)
        there = pl.ds(pl.multiple_of(me_y * own + index * 32, 32), 32)
        values = (
            tok_ref[at, :].astype(jnp.float32)
            + part[there, :].astype(jnp.float32)
            + part_y[at, :].astype(jnp.float32)
        )
        mid_ref[at, :] = values
        scale = lax.rsqrt(jnp.mean(values * values, axis=-1, keepdims=True) + epsilon)
        n2_ref[there, :] = (values * scale * gain_ref[1:2, :]).astype(jnp.bfloat16)
        return carry

    lax.fori_loop(0, own // 32, middle, 0)
    n2_y.start()
    hand_if(inner, (0, 3))
    hand_if(outer, (1, 1), (1, 3))
    pass_if(outer, 3)
    cross(0, order[2])
    hand_if(inner, (1, 3), (2, 3))
    hand_if(outer, (2, 1), (2, 3))
    cross(0, order[1])
    cross(1, order[2])
    cross(1, order[1])
    cross(2, order[2])
    cross(2, order[1])
    for kind in range(3):
        cross(kind, order[3])
    for kind in range(3):
        for step in range(z_size):
            for far in range(2):
                f_c_in(kind, step, far).wait_recv()
    for step in range(z_size):
        d_y_in(step).wait_recv()
    n2_y_in.wait_recv()

    for kind in range(3):
        a_z_done(kind)
    d_z_done()
    tok_y.wait_send()
    part_out.wait_send()
    n2_y.wait_send()
    own_d.wait()
    for copy in saves:
        copy.wait()
    for step in range(z_size):
        d_y(step).wait_send()
        for far in range(2):
            kv_y(step, far).wait_send()
        for kind in range(3):
            if step:
                f_z(kind, step, lambda copy: copy.wait_send())
            a_x(kind, step).wait_send()
            f_x_done(kind, step)
            for far in range(2):
                a_c(kind, step, far).wait_send()
                f_c(kind, step, far).wait_send()


def pre_call(
    tokens, w_kv, gain_one, gain_two, table, segments, cotangent, w_query, w_out, ffn
):
    z_size = lax.axis_size("z")
    own, width = tokens.shape
    seq = 2 * own
    rows, cols = w_query.shape
    head = table[0].shape[1] * 2
    units = ragged_split(ffn[0].shape[1], z_size)[1]
    low = lambda *dims: jax.ShapeDtypeStruct(dims, jnp.bfloat16)
    full = lambda *dims: jax.ShapeDtypeStruct(dims, jnp.float32)
    dma = lambda *lead: pltpu.SemaphoreType.DMA(lead)
    vmem = pl.BlockSpec(memory_space=pltpu.VMEM)
    hbm = pl.BlockSpec(memory_space=pl.ANY)
    wide = lambda *lead: pltpu.VMEM((*lead, width), jnp.bfloat16)
    return pl.pallas_call(
        functools.partial(pre_kernel, z_size),
        out_shape=(
            low(seq, width),
            low(seq, cols),
            low(seq, head),
            low(seq, head),
            low(seq, cols),
            full(own, width),
            low(seq, width),
            full(8, width),
            full(seq, seq),
            low(width, 2 * head + 128),
            low(width, cols),
            low(width, cols),
            low(3, width, units),
            low(z_size, seq, width),
        ),
        in_specs=[vmem] * 7 + [hbm] * 6,
        out_specs=(vmem,) * 9 + (hbm,) * 5,
        scratch_shapes=[
            pltpu.VMEM((width, 2 * head + 128), jnp.bfloat16),
            pltpu.VMEM((width, cols), jnp.bfloat16),
            pltpu.VMEM((width, cols), jnp.bfloat16),
            wide(seq),
            wide(seq),
            wide(own),
            pltpu.VMEM((seq, cols), jnp.float32),
            pltpu.VMEM((128, 128), jnp.float32),
            dma(4),
            dma(4),
            dma(2 * z_size),
            dma(2 * z_size),
            dma(3, z_size + 1),
            dma(3, z_size),
            dma(3, z_size),
            dma(3, z_size),
            dma(3, 2 * z_size),
            dma(3, 2 * z_size),
            dma(3, z_size, 2),
            dma(3, z_size, 2),
            dma(3, z_size),
            dma(3, z_size),
            dma(3, 2 * z_size),
            dma(3, 2 * z_size),
            dma(z_size + 1),
            dma(z_size),
            dma(z_size),
            dma(z_size),
            dma(16),
        ],
        compiler_params=pltpu.CompilerParams(
            collective_id=1, has_side_effects=True, vmem_limit_bytes=VMEM_BYTES
        ),
        cost_estimate=pl.CostEstimate(
            flops=8 * seq * width * cols,
            bytes_accessed=8 * width * (cols + units),
            transcendentals=seq * seq * cols // head,
        ),
    )(tokens, w_kv, gain_one, gain_two, *table, segments, cotangent, w_query, w_out, *ffn)


def post_kernel(
    z_size,
    main,
    tok_ref,
    gain_ref,
    gain_part_ref,
    n1_ref,
    rot_ref,
    key_ref,
    val_ref,
    att_ref,
    cos_ref,
    sin_ref,
    allow_ref,
    kv_hbm,
    wq_hbm,
    wo_hbm,
    mix_hbm,
    gmf_hbm,
    gmb_hbm,
    mid_hbm,
    sums_hbm,
    mixed_ref,
    tgrad_ref,
    gsum_ref,
    kvg_ref,
    qg_ref,
    og_ref,
    ffn_out,
    kv_w,
    q_w,
    o_w,
    o_part,
    gm,
    gm_f,
    gq,
    gkv,
    kv_sum,
    back_y,
    mix_y,
    mix_z,
    mix_s,
    o_c,
    o_x,
    o_z,
    q_c,
    q_x,
    q_z,
    kv_y,
    kv_c,
    kv_x,
    kv_z,
    gain_own,
    gain_in,
    ffn_in,
    ffn_own,
    load_sem,
    own_sem,
    fx_send,
    fx_recv,
    fz_send,
    fz_recv,
    y_send,
    y_recv,
    my_send,
    my_recv,
    mz_send,
    mz_recv,
    wc_send,
    wc_recv,
    wx_send,
    wx_recv,
    wz_send,
    wz_recv,
    kc_send,
    kc_recv,
    kz_send,
    kz_recv,
    g_send,
    g_recv,
):
    me_z, me_x = lax.axis_index("z"), lax.axis_index("x")
    me_c, me_y = lax.axis_index("c"), lax.axis_index("mp")
    own, width = tok_ref.shape
    seq = 2 * own
    head = key_ref.shape[1]
    cols_here = att_ref.shape[1]
    heads = cols_here // head
    rows = qg_ref.shape[0]
    span = width // z_size
    mine = pl.ds(pl.multiple_of(me_y * own, own), own)
    theirs = pl.ds(pl.multiple_of((1 - me_y) * own, own), own)
    to_y, to_x, to_c = {"mp": 1 - me_y}, {"x": 1 - me_x}, {"c": 1 - me_c}
    head_scale = head ** (-0.5)

    def behind(step):
        return lax.rem(me_z - step + z_size, z_size)

    def to_z(step):
        return {"z": lax.rem(me_z + step, z_size)}

    def row_block(step, x_at, c_at):
        start = ((behind(step) * 2 + x_at) * 2 + c_at) * rows
        return pl.ds(pl.multiple_of(start, rows), rows)

    loads = [
        pltpu.make_async_copy(wo_hbm, o_w, load_sem.at[0]),
        pltpu.make_async_copy(wq_hbm, q_w, load_sem.at[1]),
        pltpu.make_async_copy(
            kv_hbm.at[:, :, :, :, :, pl.ds(0, 2 * head)], kv_w, load_sem.at[2]
        ),
    ]
    for step in range(z_size):
        loads.append(
            pltpu.make_async_copy(mix_hbm.at[step, me_y], mix_s.at[step], load_sem.at[3 + step])
        )
    loads.append(pltpu.make_async_copy(gmf_hbm, gm_f, load_sem.at[3 + z_size]))
    loads.append(pltpu.make_async_copy(gmb_hbm, gm.at[mine], load_sem.at[4 + z_size]))
    mid_load = pltpu.make_async_copy(mid_hbm, gm_f, load_sem.at[5 + z_size])
    for load in loads:
        load.start()

    barrier = pltpu.get_barrier_semaphore()
    peers = [to_y, to_x, to_c] + [to_z(step) for step in range(1, z_size)]
    for where in peers:
        pl.semaphore_signal(barrier, inc=1, device_id=where, device_id_type=MESH_ID)
    pl.semaphore_wait(barrier, len(peers))

    tasks = [(step, kind) for step in (2, 3) for kind in range(3)]

    def f_x(index):
        step, kind = tasks[index]
        return remote(
            sums_hbm.at[kind, step, 1],
            ffn_in.at[index],
            fx_send.at[index],
            fx_recv.at[index],
            to_x,
        )

    def f_own(index):
        step, kind = tasks[index]
        return pltpu.make_async_copy(
            sums_hbm.at[kind, step, 0], ffn_own.at[index % 2], own_sem.at[index % 2]
        )

    def f_z(step, kind, source_z, act):
        for case, columns in (
            ((source_z > 0) & (source_z < z_size - 1), ffn_out.shape[3]),
            ((source_z == 0) | (source_z == z_size - 1), main),
        ):

            @pl.when(case)
            def _(columns=columns):
                cols = pl.ds(0, columns)
                if step == 1:
                    src = sums_hbm.at[kind, 1, 0, :, cols]
                else:
                    src = ffn_in.at[tasks.index((step, kind)), :, cols]
                act(
                    remote(
                        src,
                        ffn_out.at[kind, step, :, cols],
                        fz_send.at[kind, step],
                        fz_recv.at[kind, step],
                        to_z(step),
                    )
                )

    def tick(index):
        step, kind = tasks[index]
        f_x(index).wait_recv()
        f_own(index).wait()
        block = ffn_in.at[index]
        add_rows(block, [ffn_own.at[index % 2]], block, rows)
        if index + 2 < len(tasks):
            f_own(index + 2).start()
        f_z(step, kind, me_z, lambda copy: copy.start())

    def f_x_own(kind):
        return remote(
            sums_hbm.at[kind, 0, 1],
            ffn_out.at[kind, 0],
            fx_send.at[len(tasks) + kind],
            fx_recv.at[len(tasks) + kind],
            to_x,
        )

    f_own(0).start()
    f_own(1).start()
    for index in range(len(tasks)):
        f_x(index).start()
    for kind in range(3):
        f_z(1, kind, me_z, lambda copy: copy.start())

    gm_y = remote(gmb_hbm, gm.at[mine], y_send.at[0], y_recv.at[0], to_y)
    gm_y_in = remote(gm.at[theirs], gm.at[theirs], y_send.at[0], y_recv.at[0], to_y)
    gm_y.start()

    first_z, last_z = (z_size - 1 - me_z) // (z_size - 1), me_z // (z_size - 1)
    inner = first_z + last_z == 0
    order = (
        0,
        1 + (me_z + 1) // 2,
        2 + (2 * me_z - 3) * (1 - first_z - last_z),
        3 - 2 * (me_z // 2),
    )
    right = (None, 1 - me_z // 2, (3 - me_z) * (2 - me_z) // 6 + me_z // 2 * (1 - last_z), 1 - me_z // 2)

    def hop_slot(index):
        step, way = order[index], right[index]
        return way * lax.rem(step + 1, z_size) + (1 - way) * (step - 1 + 4 * ((3 - step) // 2))

    def hop_target(index):
        return {"z": me_z + 2 * right[index] - 1}

    def mix_over_y(step):
        return remote(
            mix_hbm.at[step, 1 - me_y], mix_y.at[step], my_send.at[step], my_recv.at[step], to_y
        )

    def mix_over_z(index):
        slot = hop_slot(index)
        return remote(
            mix_s.at[order[index]],
            mix_z.at[slot],
            mz_send.at[index],
            mz_recv.at[slot],
            hop_target(index),
        )

    def mix_z_in(slot):
        return remote(mix_z.at[slot], mix_z.at[slot], mz_send.at[1], mz_recv.at[slot], to_z(1))

    def mix_add(step, others, last):
        def add_tile(tile, carry):
            at = pl.ds(pl.multiple_of(tile * TILE, TILE), TILE)
            total = mix_s[step, at, :].astype(jnp.float32)
            for other in others:
                total = total + other[at, :].astype(jnp.float32)
            if last:
                mixed_ref[:, at] = (gm_f[:, at] + total.T).astype(jnp.bfloat16)
            else:
                mix_s[step, at, :] = total.astype(jnp.bfloat16)
            return carry

        lax.fori_loop(0, width // TILE, add_tile, 0)

    def mix_step(index):
        step = order[index]
        mix_over_y(step).wait_recv()
        from_y = mix_y.at[step]
        if index:

            @pl.when(inner)
            def _():
                mix_z_in(step).wait_recv()
                mix_add(step, [from_y, mix_z.at[step]], False)

            @pl.when(first_z + last_z > 0)
            def _():
                mix_add(step, [from_y], False)

            mix_over_z(index).start()
        else:
            mid_load.wait()

            @pl.when(first_z == 0)
            def _():
                mix_z_in(0).wait_recv()

            @pl.when(last_z == 0)
            def _():
                mix_z_in(z_size).wait_recv()

            @pl.when(inner)
            def _():
                mix_add(0, [from_y, mix_z.at[0], mix_z.at[z_size]], True)

            @pl.when(first_z > 0)
            def _():
                mix_add(0, [from_y, mix_z.at[z_size]], True)

            @pl.when(last_z > 0)
            def _():
                mix_add(0, [from_y, mix_z.at[0]], True)

    for index in (1, 2, 3, 0):
        mix_over_y(order[index]).start()

    kinds = ((o_part, o_c, o_x, o_z, og_ref), (o_w, q_c, q_x, q_z, qg_ref))

    def w_c(kind, step, far):
        x_at = 1 - me_x if far else me_x
        return remote(
            kinds[kind][0].at[row_block(step, x_at, 1 - me_c)],
            kinds[kind][1].at[step, far],
            wc_send.at[kind, step, far],
            wc_recv.at[kind, step, far],
            to_c,
        )

    def w_x(kind, step):
        return remote(
            kinds[kind][0].at[row_block(step, 1 - me_x, me_c)],
            kinds[kind][2].at[step],
            wx_send.at[kind, step],
            wx_recv.at[kind, step],
            to_x,
        )

    def w_z(kind, index):
        step, slot = order[index], hop_slot(index)
        return remote(
            kinds[kind][0].at[row_block(step, me_x, me_c)],
            kinds[kind][3].at[slot],
            wz_send.at[kind, index],
            wz_recv.at[kind, slot],
            hop_target(index),
        )

    def w_z_in(kind, slot):
        block = kinds[kind][3].at[slot]
        return remote(block, block, wz_send.at[kind, 1], wz_recv.at[kind, slot], to_z(1))

    def w_x_stage(kind, index):
        step = order[index]
        w_c(kind, step, 1).wait_recv()
        block = kinds[kind][0].at[row_block(step, 1 - me_x, me_c)]
        add_rows(block, [kinds[kind][1].at[step, 1]], block, rows)
        w_x(kind, step).start()

    def w_z_stage(kind, index):
        part, from_c, from_x, from_z, result = kinds[kind]
        step = order[index]
        w_c(kind, step, 0).wait_recv()
        w_x(kind, step).wait_recv()
        block = part.at[row_block(step, me_x, me_c)]
        others = [from_c.at[step, 0], from_x.at[step]]
        if index:

            @pl.when(inner)
            def _():
                w_z_in(kind, step).wait_recv()
                add_rows(block, [*others, from_z.at[step]], block, rows)

            @pl.when(first_z + last_z > 0)
            def _():
                add_rows(block, others, block, rows)

            w_z(kind, index).start()
        else:

            @pl.when(first_z == 0)
            def _():
                w_z_in(kind, 0).wait_recv()

            @pl.when(last_z == 0)
            def _():
                w_z_in(kind, z_size).wait_recv()

            @pl.when(inner)
            def _():
                add_rows(block, [*others, from_z.at[0], from_z.at[z_size]], result, rows)

            @pl.when(first_z > 0)
            def _():
                add_rows(block, [*others, from_z.at[z_size]], result, rows)

            @pl.when(last_z > 0)
            def _():
                add_rows(block, [*others, from_z.at[0]], result, rows)

    def w_product(kind, index, left, values):
        step = order[index]
        at = pl.ds(pl.multiple_of(behind(step) * span, 128), span)
        turned = left[:, at].T

        def tile_body(tile, carry):
            cols = pl.ds(pl.multiple_of(tile * TILE, TILE), TILE)
            kinds[kind][0][at, cols] = dot_nn(turned, values[:, cols]).astype(jnp.bfloat16)
            return carry

        lax.fori_loop(0, cols_here // TILE, tile_body, 0)
        for far in (1, 0):
            w_c(kind, step, far).start()

    tick(0)
    tick(1)
    loads[-1].wait()
    gm_y_in.wait_recv()
    w_product(0, 1, gm, att_ref)
    w_product(0, 2, gm, att_ref)
    w_x_stage(0, 1)
    w_product(0, 3, gm, att_ref)
    w_x_stage(0, 2)
    tick(2)
    w_product(0, 0, gm, att_ref)
    w_x_stage(0, 3)
    for load in loads[:-1]:
        load.wait()

    kv_sum[...] = jnp.zeros(kv_sum.shape, jnp.float32)
    table = (cos_ref[...], sin_ref[...])

    for index in range(2):
        cols = pl.ds(index * (cols_here // 2), cols_here // 2)
        gq[:, cols] = dot_nn(gm[...], o_w[:, cols]).astype(jnp.bfloat16)

    def attend_back(index):
        cols = pl.ds(index * head, head)
        grad_vals = gq[:, cols]
        rotated = rot_ref[:, cols]
        probs = head_probs(rotated, key_ref[...], allow_ref[...])
        grad_probs = matmul_nt(grad_vals, val_ref[...])
        delta = jnp.sum(probs * grad_probs, axis=-1, keepdims=True)
        grad_scores = (probs * (grad_probs - delta)).astype(jnp.bfloat16)
        grad_rot = dot_nn(grad_scores, key_ref[...])
        gq[:, cols] = (spin_back(grad_rot, table) * head_scale).astype(jnp.bfloat16)
        kv_sum[0] += matmul_tn(grad_scores, rotated)
        kv_sum[1] += matmul_tn(probs.astype(jnp.bfloat16), grad_vals)

    for index in range(heads):
        attend_back(index)
        if index == 0:
            w_x_stage(0, 0)
        if 3 + index < len(tasks):
            tick(3 + index)
        if index == heads - 1:
            mix_step(1)
    gkv[:, :head] = spin_back(kv_sum[0], table).astype(jnp.bfloat16)
    gkv[:, head:] = kv_sum[1].astype(jnp.bfloat16)

    w_product(1, 1, n1_ref, gq)
    w_product(1, 2, n1_ref, gq)
    w_x_stage(1, 1)
    w_z_stage(0, 1)
    w_product(1, 3, n1_ref, gq)
    w_x_stage(1, 2)
    w_product(1, 0, n1_ref, gq)
    w_x_stage(1, 3)
    w_x_stage(1, 0)
    for kind in range(3):
        f_x_own(kind).start()

    gm_y.wait_send()
    back = gm
    def input_tile(index, carry):
        at = pl.ds(pl.multiple_of(index * span, 128), span)
        back[:, at] = (
            matmul_nt(gq[...], q_w[at, :]) + matmul_nt(gkv[...], kv_w[index].reshape(span, 2 * head))
        ).astype(jnp.bfloat16)
        return carry

    lax.fori_loop(0, z_size, input_tile, 0)
    back_out = remote(back.at[theirs], back_y, y_send.at[1], y_recv.at[1], to_y)
    back_out.start()

    kv_part = kv_w

    def kv_tile(index, carry):
        at = pl.ds(pl.multiple_of(index * span, 128), span)
        product = dot_nn(n1_ref[:, at].T, gkv[...]).astype(jnp.bfloat16)
        kv_part[index] = product.reshape(kv_part.shape[1:])
        return carry

    lax.fori_loop(0, z_size, kv_tile, 0)
    kv_over_y = remote(kv_part.at[:, :, :, 1 - me_y], kv_y, y_send.at[2], y_recv.at[2], to_y)
    kv_over_y.start()
    mix_step(2)
    w_z_stage(0, 2)
    mix_step(3)
    w_z_stage(0, 3)

    back_out.wait_recv()

    def input_rows(index, total):
        at = pl.ds(pl.multiple_of(index * 32, 32), 32)
        there = pl.ds(pl.multiple_of(me_y * own + index * 32, 32), 32)
        upstream = back[there, :].astype(jnp.float32) + back_y[at, :].astype(jnp.float32)
        grad, gain_part = norm_back(
            tok_ref[at, :].astype(jnp.float32), gain_ref[0:1, :], upstream
        )
        tgrad_ref[at, :] = (gm_f[at, :] + grad).astype(jnp.bfloat16)
        return total + gain_part

    attn_gain_part = lax.fori_loop(
        0, own // 32, input_rows, jnp.zeros((1, width), jnp.float32)
    )
    for index in range(4):
        at = slice(index * span, (index + 1) * span)
        gain_own[0, index : index + 1, :] = attn_gain_part[:, at]
        gain_own[0, 4 + index : 5 + index, :] = gain_part_ref[4 + index : 5 + index, :]

    def gain_send(stage, where):
        return remote(
            gain_own.at[stage], gain_in.at[stage], g_send.at[stage], g_recv.at[stage], where
        )

    gain_hops = [gain_send(0, to_y), gain_send(1, to_c), gain_send(2, to_x)]
    gain_last = [
        remote(
            gain_own.at[3], gain_in.at[2 + step], g_send.at[2 + step], g_recv.at[2 + step], to_z(step)
        )
        for step in range(1, z_size)
    ]

    def gain_fold(stage):
        gain_hops[stage].wait_recv()
        gain_own[stage + 1] = gain_own[stage] + gain_in[stage]

    gain_hops[0].start()
    mid_load.start()
    w_z_stage(1, 1)
    w_z_stage(0, 0)
    w_z_stage(1, 2)
    gain_fold(0)
    gain_hops[1].start()
    mix_step(0)
    w_z_stage(1, 3)
    gain_fold(1)
    gain_hops[2].start()
    kv_over_y.wait_recv()

    def kv_add_y(index, carry):
        for x_at in range(2):
            for c_at in range(2):
                block = kv_part.at[index, x_at, c_at, me_y]
                block[...] = (
                    block[...].astype(jnp.float32) + kv_y[index, x_at, c_at].astype(jnp.float32)
                ).astype(jnp.bfloat16)
        return carry

    lax.fori_loop(0, z_size, kv_add_y, 0)
    kv_over_c = remote(
        kv_part.at[:, :, 1 - me_c, me_y], kv_c, kc_send.at[0], kc_recv.at[0], to_c
    )
    kv_over_c.start()
    gain_fold(2)
    for copy in gain_last:
        copy.start()
    kv_over_c.wait_recv()

    def kv_add_c(index, carry):
        for x_at in range(2):
            block = kv_part.at[index, x_at, me_c, me_y]
            block[...] = (
                block[...].astype(jnp.float32) + kv_c[index, x_at].astype(jnp.float32)
            ).astype(jnp.bfloat16)
        return carry

    lax.fori_loop(0, z_size, kv_add_c, 0)
    kv_over_x = remote(
        kv_part.at[:, 1 - me_x, me_c, me_y], kv_x, kc_send.at[1], kc_recv.at[1], to_x
    )
    kv_over_x.start()
    w_z_stage(1, 0)
    kv_over_x.wait_recv()

    def kv_add_x(index, carry):
        block = kv_part.at[index, me_x, me_c, me_y]
        block[...] = (
            block[...].astype(jnp.float32) + kv_x[index].astype(jnp.float32)
        ).astype(jnp.bfloat16)
        return carry

    lax.fori_loop(0, z_size, kv_add_x, 0)
    kv_over_z = [
        remote(
            kv_part.at[lax.rem(me_z + step, z_size), me_x, me_c, me_y],
            kv_z.at[step - 1],
            kz_send.at[step],
            kz_recv.at[step],
            to_z(step),
        )
        for step in range(1, z_size)
    ]
    for copy in kv_over_z:
        copy.start()
    for copy in gain_last:
        copy.wait_recv()
    gsum_ref[...] = gain_own[3] + gain_in[3] + gain_in[4] + gain_in[5]
    for copy in kv_over_z:
        copy.wait_recv()
    kvg_ref[...] = (
        kv_part[me_z, me_x, me_c, me_y].astype(jnp.float32)
        + kv_z[0].astype(jnp.float32)
        + kv_z[1].astype(jnp.float32)
        + kv_z[2].astype(jnp.float32)
    )

    back_out.wait_send()
    kv_over_y.wait_send()
    kv_over_c.wait_send()
    kv_over_x.wait_send()
    for kind in range(3):
        f_x_own(kind).wait()
    for index in range(len(tasks)):
        f_x(index).wait_send()
    for step in range(1, z_size):
        for kind in range(3):
            f_z(step, kind, me_z, lambda copy: copy.wait_send())
            f_z(step, kind, behind(step), lambda copy: copy.wait_recv())
    for copy in gain_hops + gain_last + kv_over_z:
        copy.wait_send()
    for step in range(z_size):
        mix_over_y(step).wait_send()
        if step:
            mix_over_z(step).wait_send()
        for kind in range(2):
            w_c(kind, step, 0).wait_send()
            w_c(kind, step, 1).wait_send()
            w_x(kind, step).wait_send()
            if step:
                w_z(kind, step).wait_send()


def post_call(
    tokens,
    gains,
    gain_part,
    normed_one,
    rotated,
    keys,
    values,
    attn_vals,
    table,
    allowed,
    kv_weight,
    query_weight,
    out_weight,
    mix_parts,
    grad_mid,
    grad_mid_low,
    mid,
    ffn_sums,
    main,
):
    z_size = lax.axis_size("z")
    own, width = tokens.shape
    seq = 2 * own
    head = keys.shape[1]
    cols = attn_vals.shape[1]
    rows = width // (4 * z_size)
    units = ffn_sums.shape[4]
    low = lambda *dims: pltpu.VMEM(dims, jnp.bfloat16)
    full = lambda *dims: pltpu.VMEM(dims, jnp.float32)
    out_full = lambda *dims: jax.ShapeDtypeStruct(dims, jnp.float32)
    out_low = lambda *dims: jax.ShapeDtypeStruct(dims, jnp.bfloat16)
    dma = lambda *lead: pltpu.SemaphoreType.DMA(lead)
    vmem = pl.BlockSpec(memory_space=pltpu.VMEM)
    hbm = pl.BlockSpec(memory_space=pl.ANY)
    z = z_size
    return pl.pallas_call(
        functools.partial(post_kernel, z_size, main),
        out_shape=(
            out_low(own, width),
            out_low(own, width),
            out_full(8, width // z),
            out_full(rows // 2, 2 * head),
            out_full(rows, cols),
            out_full(rows, cols),
            out_low(3, z, rows, units),
        ),
        in_specs=[vmem] * 11 + [hbm] * 8,
        out_specs=(vmem,) * 6 + (hbm,),
        scratch_shapes=[
            low(z, 2, 2, 2, rows // 2, 2 * head),
            low(width, cols),
            low(width, cols),
            low(width, cols),
            low(seq, width),
            full(own, width),
            low(seq, cols),
            low(seq, 2 * head),
            full(2, seq, head),
            low(own, width),
            low(z, width, own),
            low(z + 1, width, own),
            low(z, width, own),
            low(z, 2, rows, cols),
            low(z, rows, cols),
            low(z + 1, rows, cols),
            low(z, 2, rows, cols),
            low(z, rows, cols),
            low(z + 1, rows, cols),
            low(z, 2, 2, rows // 2, 2 * head),
            low(z, 2, rows // 2, 2 * head),
            low(z, rows // 2, 2 * head),
            low(z - 1, rows // 2, 2 * head),
            full(4, 8, width // z),
            full(6, 8, width // z),
            low(6, rows, units),
            low(2, rows, units),
            dma(6 + z),
            dma(2),
            dma(9),
            dma(9),
            dma(3, z),
            dma(3, z),
            dma(3),
            dma(3),
            dma(z),
            dma(z),
            dma(z),
            dma(z + 1),
            dma(2, z, 2),
            dma(2, z, 2),
            dma(2, z),
            dma(2, z),
            dma(2, z),
            dma(2, z + 1),
            dma(2),
            dma(2),
            dma(z),
            dma(z),
            dma(6),
            dma(6),
        ],
        compiler_params=pltpu.CompilerParams(
            collective_id=2, has_side_effects=True, vmem_limit_bytes=VMEM_BYTES
        ),
        cost_estimate=pl.CostEstimate(
            flops=14 * seq * width * cols,
            bytes_accessed=10 * width * cols,
            transcendentals=seq * seq * cols // head,
        ),
    )(
        tokens,
        gains,
        gain_part,
        normed_one,
        rotated,
        keys,
        values,
        attn_vals,
        *table,
        allowed,
        kv_weight.reshape(z, 2, 2, 2, rows // 2, kv_weight.shape[1]),
        query_weight,
        out_weight,
        mix_parts,
        grad_mid,
        grad_mid_low,
        mid,
        ffn_sums,
    )


def layout_kernel(
    z_size,
    main,
    sum_ref,
    ffn_ref,
    q_ref,
    o_ref,
    kv_ref,
    mixed_in,
    tgrad_in,
    wg_ref,
    wu_ref,
    wd_ref,
    qg_ref,
    og_ref,
    kvg_ref,
    mixed_ref,
    tgrad_ref,
):
    me_z = lax.axis_index("z")
    for kind, out in enumerate((wg_ref, wu_ref, wd_ref)):
        for step in range(z_size):
            at = lax.rem(me_z - step + z_size, z_size)
            values = ffn_ref[kind, step].astype(jnp.float32)
            if step == 0:
                values = values + sum_ref[kind, 0, 0].astype(jnp.float32)
            body = pl.ds(pl.multiple_of(at * main, 128), main)
            out[:, body] = values[:, :main]

            @pl.when((at > 0) & (at < z_size - 1))
            def _(out=out, at=at, values=values):
                tail = z_size * main + lax.rem(at + 1, 2) * 128
                out[:, pl.ds(pl.multiple_of(tail, 128), 128)] = values[:, main:]
    qg_ref[...] = q_ref[...]
    og_ref[...] = o_ref[...]
    kvg_ref[...] = kv_ref[...]
    mixed_ref[...] = mixed_in[...]
    tgrad_ref[...] = tgrad_in[...]


def layout_call(ffn_sums, ffn_grads, query_grad, out_grad, kv_grad, mixed, tokens_grad, ffn_cols):
    z_size = lax.axis_size("z")
    main, units = ragged_split(ffn_cols, z_size)
    rows, cols = query_grad.shape
    parts = rows // 80
    kv_rows = kv_grad.shape[0] // parts
    full = lambda *dims: jax.ShapeDtypeStruct(dims, jnp.float32)
    row = lambda height, width: pl.BlockSpec((height, width), lambda index: (index, 0))
    own, width = mixed.shape
    share = pl.BlockSpec((own, width // parts), lambda index: (0, index))
    specs = [row(80, cols), row(80, cols), row(kv_rows, kv_grad.shape[1]), share, share]
    return pl.pallas_call(
        functools.partial(layout_kernel, z_size, main),
        grid=(parts,),
        out_shape=(
            *[full(rows, ffn_cols)] * 3,
            full(rows, cols),
            full(rows, cols),
            full(*kv_grad.shape),
            jax.ShapeDtypeStruct(mixed.shape, jnp.bfloat16),
            jax.ShapeDtypeStruct(mixed.shape, jnp.bfloat16),
        ),
        in_specs=[
            pl.BlockSpec((3, 1, 1, 80, units), lambda index: (0, 0, 0, index, 0)),
            pl.BlockSpec((3, z_size, 80, units), lambda index: (0, 0, index, 0)),
            *specs,
        ],
        out_specs=(*[row(80, ffn_cols)] * 3, *specs),
        compiler_params=pltpu.CompilerParams(vmem_limit_bytes=VMEM_BYTES),
    )(ffn_sums, ffn_grads, query_grad, out_grad, kv_grad, mixed, tokens_grad)


FF_SPLIT = 4


def ffn_pass(normed, grad_out, gate_weight, up_weight, down_weight):
    gate = jnp.dot(normed, gate_weight, preferred_element_type=jnp.float32)
    up_proj = jnp.dot(normed, up_weight, preferred_element_type=jnp.float32)
    grad_hidden = jnp.dot(grad_out, down_weight, preferred_element_type=jnp.float32)
    product, pull = jax.vjp(gelu_product, gate, up_proj)
    hidden = product.astype(jnp.bfloat16)
    grad_gate_f, grad_up_f = pull(grad_hidden)
    grad_gate = grad_gate_f.astype(jnp.bfloat16)
    grad_up = grad_up_f.astype(jnp.bfloat16)
    mixed_part = matmul_nt(hidden, down_weight).astype(jnp.bfloat16)
    normed_part = (matmul_nt(grad_gate, gate_weight) + matmul_nt(grad_up, up_weight)).astype(
        jnp.bfloat16
    )
    weight_parts = [
        matmul_tn(normed, grad_gate).astype(jnp.bfloat16),
        matmul_tn(normed, grad_up).astype(jnp.bfloat16),
        matmul_tn(grad_out, hidden).astype(jnp.bfloat16),
    ]
    return mixed_part, normed_part, weight_parts


def shards_general(
    tokens,
    segments,
    positions,
    cotangent,
    attn_gain,
    ffn_gain,
    w_kv,
    w_query,
    w_out,
    w_gate,
    w_up,
    w_down,
):
    everywhere = ("z", "xc", "mp")
    dp = ("z", "xc")
    z_size = lax.axis_size("z")
    xc_size = lax.axis_size("xc")
    gains = lax.all_gather(
        jnp.stack([attn_gain, ffn_gain], axis=1), everywhere, axis=0, tiled=True
    ).astype(jnp.float32)
    gain_one, gain_two = gains[:, 0], gains[:, 1]
    kv_weight = lax.all_gather(w_kv, everywhere, axis=0, tiled=True)
    head_dim = kv_weight.shape[1] // 2
    width = tokens.shape[1]
    seq_len = segments.shape[0]
    heads_here = w_query.shape[1] // head_dim
    scale = head_dim ** (-0.5)
    cosine, sine = rotary_angles(positions, head_dim)
    inputs_f = tokens.astype(jnp.float32)
    tokens_all = lax.all_gather(tokens, "mp", axis=0, tiled=True)
    normed_one = norm_gain(tokens_all.astype(jnp.float32), gain_one).astype(jnp.bfloat16)
    query_weight = lax.all_gather(w_query, dp, axis=0, tiled=True)
    out_weight = lax.all_gather(w_out, dp, axis=0, tiled=True)

    rows = w_gate.shape[0]
    unit = w_gate.shape[1] // z_size

    def spread(weight):
        pieces = weight.reshape(rows, z_size, unit).transpose(1, 0, 2)
        pieces = lax.all_to_all(pieces, "z", split_axis=0, concat_axis=0, tiled=True)
        return lax.all_gather(pieces, "xc", axis=1, tiled=False).reshape(width, unit)

    gate_weight, up_weight, down_weight = spread(w_gate), spread(w_up), spread(w_down)
    grad_all = lax.all_gather(cotangent, ("z", "mp"), axis=0, tiled=True)

    query = jnp.dot(normed_one, query_weight, preferred_element_type=jnp.float32).reshape(
        seq_len, heads_here, head_dim
    )
    rotated = (rotate(query, cosine[:, None], sine[:, None]) * scale).astype(jnp.bfloat16)
    keyval = jnp.dot(normed_one, kv_weight, preferred_element_type=jnp.float32)
    keys = rotate(keyval[:, :head_dim], cosine, sine).astype(jnp.bfloat16)
    values = keyval[:, head_dim:].astype(jnp.bfloat16)
    allowed = block_allowed(segments, 0, seq_len)
    scores = jnp.einsum("thd,sd->hts", rotated, keys, preferred_element_type=jnp.float32)
    scores = jnp.where(allowed[None], scores, masked_score)
    row_max = jnp.max(scores, axis=-1, keepdims=True)
    weights = jnp.exp(scores - row_max)
    probs = weights / jnp.sum(weights, axis=-1, keepdims=True)
    probs_low = probs.astype(jnp.bfloat16)
    attn_vals = (
        jnp.einsum("hts,sd->thd", probs_low, values, preferred_element_type=jnp.float32)
        .reshape(seq_len, heads_here * head_dim)
        .astype(jnp.bfloat16)
    )
    mid = inputs_f + lax.psum_scatter(
        matmul_nt(attn_vals, out_weight).astype(jnp.bfloat16),
        "mp",
        scatter_dimension=0,
        tiled=True,
    ).astype(jnp.float32)
    normed_two = norm_gain(mid, gain_two).astype(jnp.bfloat16)
    normed_all = lax.all_gather(normed_two, ("z", "mp"), axis=0, tiled=True)

    mixed_part, normed_part, weight_parts = ffn_pass(
        normed_all, grad_all, gate_weight, up_weight, down_weight
    )
    grad_normed_two = lax.psum_scatter(
        normed_part, ("z", "mp"), scatter_dimension=0, tiled=True
    ).astype(jnp.float32)
    mixed = (
        mid
        + lax.psum_scatter(mixed_part, ("z", "mp"), scatter_dimension=0, tiled=True).astype(
            jnp.float32
        )
    ).astype(jnp.bfloat16)

    def collect(part):
        pieces = part.reshape(z_size, xc_size, rows, unit).transpose(1, 0, 2, 3)
        pieces = pieces.reshape(xc_size * z_size * rows, unit)
        pieces = lax.psum_scatter(pieces, "xc", scatter_dimension=0, tiled=True)
        pieces = pieces.reshape(z_size, rows, unit)
        pieces = lax.all_to_all(pieces, "z", split_axis=0, concat_axis=0, tiled=True)
        return pieces.transpose(1, 0, 2).reshape(rows, z_size * unit).astype(jnp.float32)

    w_gate_grad, w_up_grad, w_down_grad = [collect(part) for part in weight_parts]

    norm_pull_two = jax.vjp(norm_gain, mid, gain_two)[1]
    grad_mid_norm, grad_gain_two = norm_pull_two(grad_normed_two)
    grad_mid = cotangent.astype(jnp.float32) + grad_mid_norm
    grad_mid_all = lax.all_gather(grad_mid.astype(jnp.bfloat16), "mp", axis=0, tiled=True)
    grad_vals = (
        jnp.dot(grad_mid_all, out_weight, preferred_element_type=jnp.float32)
        .astype(jnp.bfloat16)
        .reshape(seq_len, heads_here, head_dim)
    )
    grad_probs = jnp.einsum("thd,sd->hts", grad_vals, values, preferred_element_type=jnp.float32)
    delta = jnp.sum(probs * grad_probs, axis=-1, keepdims=True)
    grad_scores = (probs * (grad_probs - delta)).astype(jnp.bfloat16)
    grad_rot = jnp.einsum("hts,sd->thd", grad_scores, keys, preferred_element_type=jnp.float32)
    key_sum = jnp.einsum("hts,thd->sd", grad_scores, rotated, preferred_element_type=jnp.float32)
    value_sum = jnp.einsum("hts,thd->sd", probs_low, grad_vals, preferred_element_type=jnp.float32)
    grad_query = (
        (unrotate(grad_rot, cosine[:, None], sine[:, None]) * scale)
        .reshape(seq_len, heads_here * head_dim)
        .astype(jnp.bfloat16)
    )
    grad_kv = jnp.concatenate([unrotate(key_sum, cosine, sine), value_sum], axis=1).astype(
        jnp.bfloat16
    )
    grad_normed_one = lax.psum_scatter(
        (matmul_nt(grad_query, query_weight) + matmul_nt(grad_kv, kv_weight)).astype(jnp.bfloat16),
        "mp",
        scatter_dimension=0,
        tiled=True,
    ).astype(jnp.float32)
    norm_pull_one = jax.vjp(norm_gain, inputs_f, gain_one)[1]
    grad_input_norm, grad_gain_one = norm_pull_one(grad_normed_one)
    tokens_grad = (grad_mid + grad_input_norm).astype(jnp.bfloat16)

    w_query_grad = lax.psum_scatter(
        matmul_tn(normed_one, grad_query).astype(jnp.bfloat16), dp, scatter_dimension=0, tiled=True
    ).astype(jnp.float32)
    w_out_grad = lax.psum_scatter(
        matmul_tn(grad_mid_all, attn_vals).astype(jnp.bfloat16), dp, scatter_dimension=0, tiled=True
    ).astype(jnp.float32)
    small = jnp.concatenate(
        [matmul_tn(normed_one, grad_kv), grad_gain_one[:, None], grad_gain_two[:, None]], axis=1
    )
    small = lax.psum_scatter(small, everywhere, scatter_dimension=0, tiled=True)
    kv_grad = small[:, : 2 * head_dim]
    return (
        mixed,
        tokens_grad,
        small[:, 2 * head_dim],
        small[:, 2 * head_dim + 1],
        kv_grad,
        w_query_grad,
        w_out_grad,
        w_gate_grad,
        w_up_grad,
        w_down_grad,
    )


def shards_fast(
    tokens,
    segments,
    positions,
    cotangent,
    attn_gain,
    ffn_gain,
    w_kv,
    w_query,
    w_out,
    w_gate,
    w_up,
    w_down,
):
    quarter = w_kv.shape[1] // 8
    lane = jnp.arange(2 * quarter)
    freqs = rope_base ** (-(lane % quarter).astype(jnp.float32) / quarter)
    phase = positions.astype(jnp.float32)[:, None] * freqs[None, :]
    table = (jnp.cos(phase), jnp.where(lane < quarter, -1.0, 1.0)[None, :] * jnp.sin(phase))
    (
        normed_one,
        rotated,
        keys,
        values,
        attn_vals,
        mid,
        normed_two,
        gains,
        allowed,
        kv_weight,
        query_weight,
        out_weight,
        ffn_weights,
        grad_all,
    ) = pre_call(
        tokens,
        w_kv,
        attn_gain[None, :],
        ffn_gain[None, :],
        table,
        segments[None, :],
        cotangent,
        w_query,
        w_out,
        (w_gate, w_up, w_down),
    )
    main = ragged_split(w_gate.shape[1], lax.axis_size("z"))[0]
    grad_mid, gain_part, mix_parts, ffn_sums, grad_mid_low = ffn_call(
        gains, normed_two, grad_all, ffn_weights, mid, w_gate.shape[0], main
    )
    mixed, tokens_grad, gain_grads, kv_grad, query_grad, out_grad, ffn_grads = post_call(
        tokens,
        gains,
        gain_part,
        normed_one,
        rotated,
        keys,
        values,
        attn_vals,
        table,
        allowed,
        kv_weight,
        query_weight,
        out_weight,
        mix_parts,
        grad_mid,
        grad_mid_low,
        mid,
        ffn_sums,
        main,
    )
    *ffn_out, query_grad, out_grad, kv_grad, mixed, tokens_grad = layout_call(
        ffn_sums,
        ffn_grads,
        query_grad,
        out_grad,
        kv_grad,
        mixed,
        tokens_grad,
        w_gate.shape[1],
    )
    share = attn_gain.shape[0]
    place = lax.axis_index(("z", "x", "c", "mp")) * share
    gain_grads = gain_grads.reshape(2, gain_grads.size // 2)
    gain_grads = lax.dynamic_slice(gain_grads, (0, place), (2, share))
    return (
        mixed,
        tokens_grad,
        gain_grads[0],
        gain_grads[1],
        kv_grad,
        query_grad,
        out_grad,
        *ffn_out,
    )


def solution(mesh):
    dp_size, mp_size = mesh.shape["dp"], mesh.shape["mp"]
    if dp_size == 4 * FF_SPLIT and mp_size == 2:
        body, dp = shards_fast, ("z", "x", "c")
        sizes = (FF_SPLIT, 2, 2, mp_size)
    else:
        body, dp = shards_general, ("z", "xc")
        sizes = (FF_SPLIT, dp_size // FF_SPLIT, mp_size)
    all_axes = (*dp, "mp")
    fine = jax.sharding.Mesh(mesh.devices.reshape(sizes), all_axes)
    in_specs = (
        P(all_axes, None),
        P(dp),
        P(dp),
        P(all_axes, None),
        P(all_axes),
        P(all_axes),
        P(all_axes, None),
        P(dp, "mp"),
        P(dp, "mp"),
        P(dp, "mp"),
        P(dp, "mp"),
        P(dp, "mp"),
    )
    out_specs = (
        P(all_axes, None),
        P(all_axes, None),
        P(all_axes),
        P(all_axes),
        P(all_axes, None),
        P(dp, "mp"),
        P(dp, "mp"),
        P(dp, "mp"),
        P(dp, "mp"),
        P(dp, "mp"),
    )
    return jax.shard_map(body, mesh=fine, in_specs=in_specs, out_specs=out_specs, check_vma=False)
```

```python
import functools

import jax
import jax.numpy as jnp
from jax import lax
from jax.experimental import pallas as pl
from jax.experimental.pallas import tpu as pltpu
from jax.sharding import PartitionSpec as P

WINDOW = 2048


epsilon = 1e-06
rope_base = 10000.0
masked_score = -1e30
VMEM_BYTES = 66_000_000


def norm_gain(values, gain):
    return values * lax.rsqrt(jnp.mean(values * values, axis=-1, keepdims=True) + epsilon) * gain


def rotary_angles(positions, head_width):
    quarter = head_width // 4
    freqs = rope_base ** (-jnp.arange(quarter).astype(jnp.float32) / quarter)
    phase = positions.astype(jnp.float32)[:, None] * freqs[None, :]
    return (jnp.cos(phase), jnp.sin(phase))


def rotate(values, cosine, sine):
    quarter = cosine.shape[-1]
    first_half = values[..., :quarter]
    second_half = values[..., quarter : 2 * quarter]
    return jnp.concatenate(
        [
            first_half * cosine - second_half * sine,
            second_half * cosine + first_half * sine,
            values[..., 2 * quarter :],
        ],
        axis=-1,
    )


def unrotate(values, cosine, sine):
    quarter = cosine.shape[-1]
    first_half = values[..., :quarter]
    second_half = values[..., quarter : 2 * quarter]
    return jnp.concatenate(
        [
            first_half * cosine + second_half * sine,
            second_half * cosine - first_half * sine,
            values[..., 2 * quarter :],
        ],
        axis=-1,
    )


def gelu_product(gate, up_proj):
    return jax.nn.gelu(gate, approximate=True) * up_proj


def matmul_nt(left, right):
    return lax.dot_general(
        left, right, (((1,), (1,)), ((), ())), preferred_element_type=jnp.float32
    )


def matmul_tn(left, right):
    return lax.dot_general(
        left, right, (((0,), (0,)), ((), ())), preferred_element_type=jnp.float32
    )


def block_allowed(segments, first_row, rows):
    seq_len = segments.shape[0]
    query_rows = first_row + jnp.arange(rows)
    key_rows = jnp.arange(seq_len)
    return (
        (segments[:, None] == segments[None, :])
        & (key_rows[None, :] <= query_rows[:, None])
        & (query_rows[:, None] - key_rows[None, :] < WINDOW)
    )


MESH_ID = pl.DeviceIdType.MESH
GELU_A = 0.7978845608028654
GELU_B = 0.044715
TILE = 256
WIDE = 512


def remote(src, dst, send_sem, recv_sem, where):
    return pltpu.make_async_remote_copy(
        src_ref=src,
        dst_ref=dst,
        send_sem=send_sem,
        recv_sem=recv_sem,
        device_id=where,
        device_id_type=MESH_ID,
    )


class Halves:
    def __init__(self, src, dst, send_sem, recv_sem, where):
        rows = src.shape[0] // 2
        cuts = [pl.ds(part * rows, rows) for part in range(2)]
        self.copies = [
            remote(src.at[cut], dst.at[cut], send_sem.at[part], recv_sem.at[part], where)
            for part, cut in enumerate(cuts)
        ]

    def start(self):
        for copy in self.copies:
            copy.start()

    def wait_recv(self):
        for copy in self.copies:
            copy.wait_recv()

    def wait_send(self):
        for copy in self.copies:
            copy.wait_send()


def dot_nn(left, right):
    return lax.dot_general(
        left, right, (((1,), (0,)), ((), ())), preferred_element_type=jnp.float32
    )


def gelu_parts(gate):
    square = gate * gate
    bend = jnp.tanh(GELU_A * gate * (1.0 + GELU_B * square))
    half = 0.5 * (1.0 + bend)
    slope = half + 0.5 * gate * (1.0 - bend * bend) * GELU_A * (1.0 + 3.0 * GELU_B * square)
    return gate * half, slope


def add_rows(first, rest, out, count):
    def body(index, carry):
        step = pl.ds(pl.multiple_of(index * 32, 32), 32)
        total = first[step, :].astype(jnp.float32)
        for other in rest:
            total = total + other[step, :].astype(jnp.float32)
        out[step, :] = total.astype(out.dtype)
        return carry

    lax.fori_loop(0, count // 32, body, 0)


def norm_back(values, gain, upstream):
    scale = lax.rsqrt(jnp.mean(values * values, axis=-1, keepdims=True) + epsilon)
    normed = values * scale
    pulled = gain * upstream
    back = scale * (pulled - normed * jnp.mean(normed * pulled, axis=-1, keepdims=True))
    return back, jnp.sum(upstream * normed, axis=0, keepdims=True)


def ffn_kernel(
    z_size,
    main,
    gain_ref,
    own_hbm,
    dy_hbm,
    w_hbm,
    mid_hbm,
    gm_ref,
    gain_part,
    mix_hbm,
    sums_hbm,
    gm_hbm,
    n2,
    dy,
    w3,
    h3,
    n2_t,
    dy_t,
    gn_part,
    mix_buf,
    gn_y,
    gn_z,
    gn_s,
    c_in,
    x_in,
    mid,
    load_sem,
    mix_sem,
    ag_y_send,
    ag_y_recv,
    ag_z_send,
    ag_z_recv,
    rs_y_send,
    rs_y_recv,
    rs_z_send,
    rs_z_recv,
    c_send,
    c_recv,
    x_send,
    x_recv,
    out_sem,
):
    own = own_hbm.shape[0] // 2
    width = own_hbm.shape[1]
    units = w3.shape[2]
    rows = c_in.shape[3]
    span = width // z_size
    me_y, me_z = lax.axis_index("mp"), lax.axis_index("z")
    me_x, me_c = lax.axis_index("x"), lax.axis_index("c")
    mine = pl.ds(pl.multiple_of(me_y * own, own), own)
    theirs = pl.ds(pl.multiple_of((1 - me_y) * own, own), own)
    to_y, to_x, to_c = {"mp": 1 - me_y}, {"x": 1 - me_x}, {"c": 1 - me_c}

    def ahead(step):
        return lax.rem(me_z + step, z_size)

    def to_z(step):
        return {"z": ahead(step)}

    def row_block(z_at, x_at, c_at):
        return pl.ds(pl.multiple_of(((z_at * 2 + x_at) * 2 + c_at) * rows, rows), rows)

    inner = (me_z > 0) & (me_z < z_size - 1)
    outer = (me_z == 0) | (me_z == z_size - 1)

    def w_load(index, columns):
        cols = pl.ds(0, columns)
        return pltpu.make_async_copy(
            w_hbm.at[index, :, cols], w3.at[index, :, cols], load_sem.at[z_size + index]
        )

    def w_loads(act):
        for case, columns in ((inner, units), (outer, main)):

            @pl.when(case)
            def _(columns=columns):
                for index in range(3):
                    act(w_load(index, columns))

    w_loads(lambda copy: copy.start())
    dy_loads = [
        pltpu.make_async_copy(dy_hbm.at[index], dy, load_sem.at[index])
        for index in range(z_size)
    ]
    own_load = pltpu.make_async_copy(own_hbm, n2.at[0], load_sem.at[z_size + 3])
    mid_load = pltpu.make_async_copy(mid_hbm, mid, load_sem.at[z_size + 4])
    for load in (own_load, dy_loads[0], mid_load):
        load.start()

    barrier = pltpu.get_barrier_semaphore()
    peers = [to_y, to_x, to_c] + [to_z(step) for step in range(1, z_size)]
    for where in peers:
        pl.semaphore_signal(barrier, inc=1, device_id=where, device_id_type=MESH_ID)
    pl.semaphore_wait(barrier, len(peers))

    def ag_y(index):
        block = n2.at[index, mine]
        return Halves(block, block, ag_y_send.at[index], ag_y_recv.at[index], to_y)

    def ag_y_in(index):
        block = n2.at[index, theirs]
        return Halves(block, block, ag_y_send.at[index], ag_y_recv.at[index], to_y)

    def ag_z(index):
        src = own_hbm.at[mine] if index == 0 else n2.at[index, mine]
        return Halves(
            src, n2.at[index + 1, mine], ag_z_send.at[index], ag_z_recv.at[index + 1], to_z(1)
        )

    def ag_z_in(index):
        block = n2.at[index, mine]
        return Halves(block, block, ag_z_send.at[0], ag_z_recv.at[index], to_z(1))

    def ag_last():
        return Halves(
            n2.at[2, theirs], n2.at[3, theirs], ag_y_send.at[3], ag_y_recv.at[3], to_z(1)
        )

    def forward(index):
        ag_z_in(index).wait_recv()
        ag_z(index).start()
        ag_y(index).start()

    ag_z(0).start()

    mix_copies = []

    def turn(source, target, index):
        def turn_tile(tile, carry):
            at = pl.ds(pl.multiple_of(tile * span, 128), span)
            target[at, pl.ds(index * 2 * own, 2 * own)] = source[:, at].T
            return carry

        lax.fori_loop(0, z_size, turn_tile, 0)

    def chunk(index):
        if index:
            mix_copies[index - 1].wait()
        dy_loads[index].wait()
        rows_at = pl.ds(index * 2 * own, 2 * own)

        def up_tile(tile, carry):
            cols = pl.ds(pl.multiple_of(tile * WIDE, WIDE), WIDE)
            gate = dot_nn(n2[index], w3[0, :, cols])
            up_proj = dot_nn(n2[index], w3[1, :, cols])
            grad_hidden = dot_nn(dy[...], w3[2, :, cols])
            act, slope = gelu_parts(gate)
            h3[0, rows_at, cols] = (grad_hidden * up_proj * slope).astype(jnp.bfloat16)
            h3[1, rows_at, cols] = (grad_hidden * act).astype(jnp.bfloat16)
            h3[2, rows_at, cols] = (act * up_proj).astype(jnp.bfloat16)
            return carry

        lax.fori_loop(0, units // WIDE, up_tile, 0)

        def down_tile(tile, carry):
            at = pl.ds(pl.multiple_of(tile * span, 128), span)
            normed = matmul_nt(w3[0, at, :], h3[0, rows_at, :]) + matmul_nt(
                w3[1, at, :], h3[1, rows_at, :]
            )
            mixed = matmul_nt(w3[2, at, :], h3[2, rows_at, :])
            for half in range(2):
                cols = slice(half * own, (half + 1) * own)
                gn_part[index, half, at, :] = normed[:, cols].astype(jnp.bfloat16)
                mix_buf[half, at, :] = mixed[:, cols].astype(jnp.bfloat16)
            return carry

        lax.fori_loop(0, z_size, down_tile, 0)
        copy = pltpu.make_async_copy(mix_buf, mix_hbm.at[index], mix_sem.at[index])
        copy.start()
        mix_copies.append(copy)
        if index:
            rs_y(index).start()
        turn(n2.at[index], n2_t, index)
        turn(dy, dy_t, index)
        if index + 1 < z_size:
            dy_loads[index + 1].start()

    def rs_y(index):
        return Halves(
            gn_part.at[index, 1 - me_y], gn_y.at[index], rs_y_send.at[index], rs_y_recv.at[index], to_y
        )

    def rs_z(index):
        return Halves(
            gn_s.at[index - 1],
            gn_z.at[index - 1],
            rs_z_send.at[index],
            rs_z_recv.at[index - 1],
            to_z(1),
        )

    def rs_step(index):
        rs_y(index).wait_recv()
        slot = (index - 2) % z_size
        if index != 1:
            Halves(
                gn_s.at[slot], gn_z.at[slot], rs_z_send.at[1], rs_z_recv.at[slot], to_z(1)
            ).wait_recv()

        def add_tile(tile, carry):
            at = pl.ds(pl.multiple_of(tile * TILE, TILE), TILE)
            total = gn_part[index, me_y, at, :].astype(jnp.float32) + gn_y[index, at, :].astype(
                jnp.float32
            )
            if index != 1:
                total = total + gn_z[slot, at, :].astype(jnp.float32)
            if index == 0:
                gm_ref[:, at] = total.T
            else:
                gn_s[index - 1, at, :] = total.astype(jnp.bfloat16)
            return carry

        lax.fori_loop(0, width // TILE, add_tile, 0)
        if index != 0:
            rs_z(index).start()


    def grads(step):
        at = pl.ds(pl.multiple_of(ahead(step) * span, 128), span)
        for kind, source in enumerate((n2_t, n2_t, dy_t)):

            def tile_body(tile, carry, kind=kind, source=source):
                cols = pl.ds(pl.multiple_of(tile * WIDE, WIDE), WIDE)
                w3[kind, at, cols] = dot_nn(source[at, :], h3[kind, :, cols]).astype(jnp.bfloat16)
                return carry

            lax.fori_loop(0, units // WIDE, tile_body, 0)
            for far in (1, 0):
                over_c(kind, step, far).start()

    def over_c(kind, step, far):
        x_at = 1 - me_x if far else me_x
        return remote(
            w3.at[kind, row_block(ahead(step), x_at, 1 - me_c)],
            c_in.at[kind, step, far],
            c_send.at[kind, step, far],
            c_recv.at[kind, step, far],
            to_c,
        )

    def over_x(kind):
        return remote(
            w3.at[kind, row_block(ahead(1), 1 - me_x, me_c)],
            x_in.at[kind],
            x_send.at[kind],
            x_recv.at[kind],
            to_x,
        )

    out_copies = []

    def keep(kind, step, far, block):
        copy = pltpu.make_async_copy(
            block, sums_hbm.at[kind, step, far], out_sem.at[kind, step, far]
        )
        copy.start()
        out_copies.append(copy)

    def core_sums(step):
        pairs = [(kind, far) for kind in range(3) for far in (1, 0)]
        if step == 1:
            pairs.sort(key=lambda pair: -pair[1])
        for kind, far in pairs:
            over_c(kind, step, far).wait_recv()
            x_at = 1 - me_x if far else me_x
            block = w3.at[kind, row_block(ahead(step), x_at, me_c)]
            add_rows(block, [c_in.at[kind, step, far]], block, rows)
            if step != 1:
                keep(kind, step, far, block)
            elif far:
                over_x(kind).start()

    def first_sums():
        for kind in range(3):
            over_x(kind).wait_recv()
            block = w3.at[kind, row_block(ahead(1), me_x, me_c)]
            add_rows(block, [x_in.at[kind]], block, rows)
            keep(kind, 1, 0, block)

    own_load.wait()
    w_loads(lambda copy: copy.wait())

    @pl.when(outer)
    def _():
        w3[:, :, main:] = jnp.zeros((3, width, units - main), jnp.bfloat16)

    chunk(0)
    forward(1)
    forward(2)
    ag_y_in(1).wait_recv()
    chunk(1)
    ag_y_in(2).wait_recv()
    ag_last().start()
    chunk(2)
    rs_step(1)
    ag_z_in(3).wait_recv()
    ag_last().wait_recv()
    chunk(3)
    rs_y(0).start()
    rs_step(2)
    grads(1)
    grads(2)
    core_sums(1)
    rs_step(3)
    grads(3)
    core_sums(2)
    grads(0)
    core_sums(3)
    rs_step(0)
    core_sums(0)

    cot_load = pltpu.make_async_copy(
        dy_hbm.at[0, mine], dy.at[pl.ds(0, own)], load_sem.at[z_size + 3]
    )
    cot_load.start()
    cot_load.wait()
    mid_load.wait()

    def mid_rows(index, total):
        at = pl.ds(pl.multiple_of(index * 32, 32), 32)
        grad, gain_sum = norm_back(mid[at, :], gain_ref[1:2, :], gm_ref[at, :])
        grad = grad + dy[at, :].astype(jnp.float32)
        gm_ref[at, :] = grad
        dy[pl.ds(pl.multiple_of(own + index * 32, 32), 32), :] = grad.astype(jnp.bfloat16)
        return total + gain_sum

    gain_sum = lax.fori_loop(0, own // 32, mid_rows, jnp.zeros((1, width), jnp.float32))
    gm_save = pltpu.make_async_copy(dy.at[pl.ds(own, own)], gm_hbm, load_sem.at[z_size + 3])
    gm_save.start()
    for index in range(4):
        gain_part[index : index + 1, :] = jnp.zeros((1, span), jnp.float32)
        gain_part[4 + index : 5 + index, :] = gain_sum[:, index * span : (index + 1) * span]
    first_sums()
    gm_save.wait()

    for copy in mix_copies[3:] + out_copies:
        copy.wait()
    for index in range(z_size):
        if index in (1, 2):
            ag_y(index).wait_send()
        if index == 3:
            ag_last().wait_send()
        rs_y(index).wait_send()
        if index < z_size - 1:
            ag_z(index).wait_send()
        if index:
            rs_z(index).wait_send()
        for kind in range(3):
            over_c(kind, index, 0).wait_send()
            over_c(kind, index, 1).wait_send()
            if index == 1:
                over_x(kind).wait_send()


def ffn_call(gains, normed, grad_all, weights, mid, rows, main):
    z_size = lax.axis_size("z")
    pair, width = normed.shape
    units = weights.shape[2]
    own = pair // 2
    wide = lambda *lead: pltpu.VMEM((*lead, width), jnp.bfloat16)
    tall = lambda *lead: pltpu.VMEM((*lead, width, own), jnp.bfloat16)
    dma = lambda *lead: pltpu.SemaphoreType.DMA(lead)
    vmem = pl.BlockSpec(memory_space=pltpu.VMEM)
    hbm = pl.BlockSpec(memory_space=pl.ANY)
    return pl.pallas_call(
        functools.partial(ffn_kernel, z_size, main),
        out_shape=(
            jax.ShapeDtypeStruct((own, width), jnp.float32),
            jax.ShapeDtypeStruct((8, width // z_size), jnp.float32),
            jax.ShapeDtypeStruct((z_size, 2, width, own), jnp.bfloat16),
            jax.ShapeDtypeStruct((3, z_size, 2, rows, units), jnp.bfloat16),
            jax.ShapeDtypeStruct((own, width), jnp.bfloat16),
        ),
        in_specs=[vmem, hbm, hbm, hbm, hbm],
        out_specs=(vmem, vmem, hbm, hbm, hbm),
        scratch_shapes=[
            wide(z_size, pair),
            wide(pair),
            pltpu.VMEM(weights.shape, jnp.bfloat16),
            pltpu.VMEM((3, z_size * pair, units), jnp.bfloat16),
            pltpu.VMEM((width, z_size * pair), jnp.bfloat16),
            pltpu.VMEM((width, z_size * pair), jnp.bfloat16),
            tall(z_size, 2),
            tall(2),
            tall(z_size),
            tall(z_size - 1),
            tall(z_size - 1),
            pltpu.VMEM((3, z_size, 2, rows, units), jnp.bfloat16),
            pltpu.VMEM((3, rows, units), jnp.bfloat16),
            pltpu.VMEM((own, width), jnp.float32),
            dma(z_size + 5),
            dma(z_size),
            dma(z_size, 2),
            dma(z_size, 2),
            dma(z_size, 2),
            dma(z_size, 2),
            dma(z_size, 2),
            dma(z_size, 2),
            dma(z_size, 2),
            dma(z_size, 2),
            dma(3, z_size, 2),
            dma(3, z_size, 2),
            dma(3),
            dma(3),
            dma(3, z_size, 2),
        ],
        compiler_params=pltpu.CompilerParams(
            collective_id=0, has_side_effects=True, vmem_limit_bytes=VMEM_BYTES
        ),
        cost_estimate=pl.CostEstimate(
            flops=18 * z_size * pair * width * units,
            bytes_accessed=4 * weights.size + 12 * z_size * pair * width,
            transcendentals=z_size * pair * units,
        ),
    )(gains, normed, grad_all, weights, mid)


def spin(values, table):
    first = values[:, : values.shape[1] // 2]
    turned = first * table[0] + pltpu.roll(first, first.shape[1] // 2, 1) * table[1]
    return jnp.concatenate([turned, values[:, values.shape[1] // 2 :]], axis=1)


def spin_back(values, table):
    first = values[:, : values.shape[1] // 2]
    turned = first * table[0] - pltpu.roll(first, first.shape[1] // 2, 1) * table[1]
    return jnp.concatenate([turned, values[:, values.shape[1] // 2 :]], axis=1)


def head_probs(rotated, keys, allowed):
    scores = jnp.where(allowed > 0.5, matmul_nt(rotated, keys), masked_score)
    weights = jnp.exp(scores - jnp.max(scores, axis=-1, keepdims=True))
    return weights / jnp.sum(weights, axis=-1, keepdims=True)


def ragged_split(columns, parts):
    main = columns // parts // 128 * 128
    return main, main + 128


def pre_kernel(
    z_size,
    tok_ref,
    wkv_ref,
    gain_one_ref,
    gain_two_ref,
    cos_ref,
    sin_ref,
    seg_ref,
    cot_hbm,
    wq_hbm,
    wo_hbm,
    wg_hbm,
    wu_hbm,
    wd_hbm,
    n1_ref,
    rot_ref,
    key_ref,
    val_ref,
    att_ref,
    mid_ref,
    n2_ref,
    gain_ref,
    allow_ref,
    kv_out,
    wq_out,
    wo_out,
    w3_out,
    dy_out,
    kv_w,
    q_w,
    o_w,
    tok,
    part,
    part_y,
    query,
    gain_rows,
    y_send,
    y_recv,
    ky_send,
    ky_recv,
    az_send,
    az_recv,
    ax_send,
    ax_recv,
    ac_send,
    ac_recv,
    fz_send,
    fz_recv,
    fx_send,
    fx_recv,
    fc_send,
    fc_recv,
    dz_send,
    dz_recv,
    dy_send,
    dy_recv,
    local_sem,
):
    me_z, me_x = lax.axis_index("z"), lax.axis_index("x")
    me_c, me_y = lax.axis_index("c"), lax.axis_index("mp")
    own, width = tok_ref.shape
    rows = wq_hbm.shape[0]
    half_rows = wkv_ref.shape[0]
    head = key_ref.shape[1]
    main, units = ragged_split(wg_hbm.shape[1], z_size)
    to_y, to_x, to_c = {"mp": 1 - me_y}, {"x": 1 - me_x}, {"c": 1 - me_c}

    def to_z(step):
        return {"z": lax.rem(me_z + step, z_size)}

    def from_z(step):
        return lax.rem(me_z - step + z_size, z_size)

    def row_block(step, x_at, c_at):
        start = ((from_z(step) * 2 + x_at) * 2 + c_at) * rows
        return pl.ds(pl.multiple_of(start, rows), rows)

    mine = pl.ds(pl.multiple_of(me_y * own, own), own)
    theirs = pl.ds(pl.multiple_of((1 - me_y) * own, own), own)
    bufs = (kv_w, q_w, o_w)
    inputs = (None, wq_hbm, wo_hbm)

    locals_ = []

    def local(src, dst):
        copy = pltpu.make_async_copy(src, dst, local_sem.at[len(locals_)])
        copy.start()
        locals_.append(copy)
        return copy

    here = row_block(0, me_x, me_c)
    own_q = local(wq_hbm, q_w.at[here])
    own_o = local(wo_hbm, o_w.at[here])
    ffn_in = (wg_hbm, wu_hbm, wd_hbm)

    def body_of(target):
        return pl.ds(pl.multiple_of(target * main, 128), main), pl.ds(0, main)

    def tail_of(target):
        start = z_size * main + lax.rem(target + 1, 2) * 128
        return pl.ds(pl.multiple_of(start, 128), 128), pl.ds(main, 128)

    def is_inner(at):
        return (at > 0) & (at < z_size - 1)

    own_f = []
    for kind in range(3):
        src, dst = body_of(me_z)
        own_f.append(local(ffn_in[kind].at[:, src], w3_out.at[kind, here, dst]))

    def own_tail(kind):
        src, dst = tail_of(me_z)
        return pltpu.make_async_copy(
            ffn_in[kind].at[:, src], w3_out.at[kind, here, dst], local_sem.at[12 + kind]
        )

    @pl.when(is_inner(me_z))
    def _():
        for kind in range(3):
            own_tail(kind).start()
    own_d = local(cot_hbm, dy_out.at[0, mine])

    kv_own = pl.ds(pl.multiple_of(here.start + me_y * half_rows, half_rows), half_rows)
    gain_rows[...] = jnp.zeros(gain_rows.shape, jnp.float32)
    gain_rows[0:1, :half_rows] = gain_one_ref[...].astype(jnp.float32)
    gain_rows[1:2, :half_rows] = gain_two_ref[...].astype(jnp.float32)
    spread = gain_rows[...].T
    kv_w[kv_own, : 2 * head] = wkv_ref[...]
    kv_w[kv_own, 2 * head :] = spread[:half_rows, :].astype(jnp.bfloat16)

    barrier = pltpu.get_barrier_semaphore()
    peers = [to_y, to_x, to_c] + [to_z(step) for step in range(1, z_size)]
    for where in peers:
        pl.semaphore_signal(barrier, inc=1, device_id=where, device_id_type=MESH_ID)
    pl.semaphore_wait(barrier, len(peers))

    tok_y = remote(tok_ref, tok.at[mine], y_send.at[1], y_recv.at[1], to_y)
    tok_y_in = remote(tok_ref, tok.at[theirs], y_send.at[1], y_recv.at[1], to_y)
    part_out = remote(part.at[theirs], part_y, y_send.at[2], y_recv.at[2], to_y)
    n2_y = remote(n2_ref.at[mine], n2_ref.at[mine], y_send.at[3], y_recv.at[3], to_y)
    n2_y_in = remote(n2_ref.at[theirs], n2_ref.at[theirs], y_send.at[3], y_recv.at[3], to_y)

    def block_of(kind, step, x_at):
        if kind:
            return row_block(step, x_at, me_c)
        return kv_rows(step, x_at, me_y)

    def kv_rows(step, x_at, y_at):
        start = row_block(step, x_at, me_c).start + y_at * half_rows
        return pl.ds(pl.multiple_of(start, half_rows), half_rows)

    def kv_y(step, far):
        x_at = 1 - me_x if far else me_x
        block = kv_w.at[kv_rows(step, x_at, me_y)]
        slot = step + z_size * far
        return remote(block, block, ky_send.at[slot], ky_recv.at[slot], to_y)

    def kv_y_in(step, far):
        x_at = 1 - me_x if far else me_x
        block = kv_w.at[kv_rows(step, x_at, 1 - me_y)]
        slot = step + z_size * far
        return remote(block, block, ky_send.at[slot], ky_recv.at[slot], to_y)

    def source(kind, step):
        if isinstance(step, int) and step == 0 and kind:
            return inputs[kind]
        return bufs[kind].at[block_of(kind, step, me_x)]

    first_z, last_z = (z_size - 1 - me_z) // (z_size - 1), me_z // (z_size - 1)
    inner = first_z + last_z == 0
    order = (0, 1 + 2 * first_z, 3 - first_z - last_z, 2 - first_z + last_z)
    hops = (
        None,
        (lax.rem(me_z + 1, z_size), 2),
        (lax.rem(me_z + z_size - 1, z_size), 2),
        (lax.rem(3 * (me_z + 3), z_size), lax.rem(2 * me_z + 3, z_size)),
    )

    def a_z_own(kind, right):
        return remote(
            source(kind, 0),
            bufs[kind].at[block_of(kind, 0, me_x)],
            az_send.at[kind, right],
            az_recv.at[kind, 1 if right else z_size - 1],
            to_z(1 if right else z_size - 1),
        )

    def a_z_start(kind):
        @pl.when(last_z == 0)
        def _():
            a_z_own(kind, 1).start()

        @pl.when(first_z == 0)
        def _():
            a_z_own(kind, 0).start()

    def a_z(kind, index):
        target, slot = hops[index]
        block = bufs[kind].at[block_of(kind, order[index], me_x)]
        return remote(
            block, block, az_send.at[kind, 1 + index], az_recv.at[kind, slot], {"z": target}
        )

    def a_z_next(kind, index):
        @pl.when(inner)
        def _():
            a_z(kind, index).start()

    def a_z_done(kind):
        @pl.when(last_z == 0)
        def _():
            a_z_own(kind, 1).wait_send()

        @pl.when(first_z == 0)
        def _():
            a_z_own(kind, 0).wait_send()

        @pl.when(inner)
        def _():
            for index in range(1, z_size):
                a_z(kind, index).wait_send()

    def a_z_in(kind, step):
        block = bufs[kind].at[block_of(kind, step, me_x)]
        return remote(block, block, az_send.at[kind, 0], az_recv.at[kind, step], to_z(1))

    def a_x(kind, step):
        return remote(
            source(kind, step),
            bufs[kind].at[block_of(kind, step, me_x)],
            ax_send.at[kind, step],
            ax_recv.at[kind, step],
            to_x,
        )

    def a_x_in(kind, step):
        block = bufs[kind].at[block_of(kind, step, 1 - me_x)]
        return remote(block, block, ax_send.at[kind, step], ax_recv.at[kind, step], to_x)

    def a_c(kind, step, far):
        x_at = 1 - me_x if far else me_x
        block = bufs[kind].at[row_block(step, x_at, me_c)]
        src = source(kind, step) if kind and not far else block
        slot = step + z_size * far
        return remote(src, block, ac_send.at[kind, slot], ac_recv.at[kind, slot], to_c)

    def a_c_in(kind, step, far):
        x_at = 1 - me_x if far else me_x
        block = bufs[kind].at[row_block(step, x_at, 1 - me_c)]
        slot = step + z_size * far
        return remote(block, block, ac_send.at[kind, slot], ac_recv.at[kind, slot], to_c)

    def f_z(kind, step, act):
        target = lax.rem(me_z + step, z_size)

        def piece(index, src, dst):
            return remote(
                ffn_in[kind].at[:, src],
                w3_out.at[kind, here, dst],
                fz_send.at[kind, step, index],
                fz_recv.at[kind, step, index],
                to_z(step),
            )

        act(piece(0, *body_of(target)))

        @pl.when(is_inner(target))
        def _():
            act(piece(1, *tail_of(target)))

    def f_z_wait(kind, step):
        block = row_block(step, me_x, me_c)

        def piece(index, dst):
            part = w3_out.at[kind, block, dst]
            return remote(
                part, part, fz_send.at[kind, step, index], fz_recv.at[kind, step, index], to_z(step)
            )

        piece(0, pl.ds(0, main)).wait_recv()

        @pl.when(inner)
        def _():
            piece(1, pl.ds(main, 128)).wait_recv()

    def f_x(kind, step, x_at, act):
        for case, columns in ((inner, units), (first_z + last_z > 0, main)):

            @pl.when(case)
            def _(columns=columns):
                block = w3_out.at[kind, row_block(step, x_at, me_c), pl.ds(0, columns)]
                act(remote(block, block, fx_send.at[kind, step], fx_recv.at[kind, step], to_x))

    def f_x_start(kind, step):
        f_x(kind, step, me_x, lambda copy: copy.start())

    def f_x_wait(kind, step):
        f_x(kind, step, 1 - me_x, lambda copy: copy.wait_recv())

    def f_x_done(kind, step):
        f_x(kind, step, me_x, lambda copy: copy.wait_send())

    def f_c(kind, step, far):
        block = w3_out.at[kind, row_block(step, 1 - me_x if far else me_x, me_c)]
        slot = step + z_size * far
        return remote(block, block, fc_send.at[kind, slot], fc_recv.at[kind, slot], to_c)

    def f_c_in(kind, step, far):
        block = w3_out.at[kind, row_block(step, 1 - me_x if far else me_x, 1 - me_c)]
        slot = step + z_size * far
        return remote(block, block, fc_send.at[kind, slot], fc_recv.at[kind, slot], to_c)

    def d_source(step):
        return cot_hbm if isinstance(step, int) else dy_out.at[step, mine]

    def d_z_own(right):
        slot = 1 if right else z_size - 1
        return remote(
            cot_hbm, dy_out.at[slot, mine], dz_send.at[right], dz_recv.at[slot], to_z(slot)
        )

    def d_z_start():
        @pl.when(last_z == 0)
        def _():
            d_z_own(1).start()

        @pl.when(first_z == 0)
        def _():
            d_z_own(0).start()

    def d_z(index):
        target, slot = hops[index]
        return remote(
            dy_out.at[order[index], mine],
            dy_out.at[slot, mine],
            dz_send.at[1 + index],
            dz_recv.at[slot],
            {"z": target},
        )

    def d_z_done():
        @pl.when(last_z == 0)
        def _():
            d_z_own(1).wait_send()

        @pl.when(first_z == 0)
        def _():
            d_z_own(0).wait_send()

        @pl.when(inner)
        def _():
            for index in range(1, z_size):
                d_z(index).wait_send()

    def d_z_in(step):
        block = dy_out.at[step, mine]
        return remote(block, block, dz_send.at[0], dz_recv.at[step], to_z(1))

    def d_y(step):
        return remote(
            d_source(step), dy_out.at[step, mine], dy_send.at[step], dy_recv.at[step], to_y
        )

    def d_y_in(step):
        block = dy_out.at[step, theirs]
        return remote(block, block, dy_send.at[step], dy_recv.at[step], to_y)

    for kind in (1, 0, 2):
        a_z_start(kind)
        a_x(kind, 0).start()
    kv_y(0, 0).start()
    tok_y.start()
    for kind in (1, 2):
        a_c(kind, 0, 0).start()

    for at_end, away in ((first_z, 1), (last_z, z_size - 1)):

        @pl.when(at_end > 0)
        def _(away=away):
            for kind in range(3):
                f_z(kind, away, lambda copy: copy.start())

    tok[mine, :] = tok_ref[...]
    seq = 2 * own
    query_at = lax.broadcasted_iota(jnp.int32, (seq, seq), 0)
    key_at = lax.broadcasted_iota(jnp.int32, (seq, seq), 1)
    segment = seg_ref[...].astype(jnp.float32)
    same = jnp.broadcast_to(segment, (8, seq)).T[:, :1] == segment
    allowed = same & (key_at <= query_at) & (query_at - key_at < WINDOW)
    allow_ref[...] = jnp.where(allowed, 1.0, 0.0)
    d_y(0).start()

    def from_x(index):
        step = order[index]
        for kind in (1, 0, 2):
            a_x_in(kind, step).wait_recv()
            if kind:
                a_c(kind, step, 1).start()
            else:
                kv_y(step, 1).start()

    def from_y(index):
        step = order[index]
        for far in range(2):
            kv_y_in(step, far).wait_recv()
            a_c(0, step, far).start()

    for index in range(1, z_size):
        step = order[index]
        for kind in (1, 0, 2):
            a_z_in(kind, step).wait_recv()
            a_z_next(kind, index)
            a_x(kind, step).start()
            if kind:
                a_c(kind, step, 0).start()
            else:
                kv_y(step, 0).start()
        if index == z_size - 2:
            d_z_start()
        if index == z_size - 1:
            for copy in own_f:
                copy.wait()

            @pl.when(inner)
            def _():
                for kind in range(3):
                    own_tail(kind).wait()

            for at, ways in enumerate(((3, 2), (3, 2, 1), (1, 2, 3), (1, 2))):

                @pl.when(me_z == at)
                def _(ways=ways):
                    for kind in range(3):
                        for away in ways:
                            f_z(kind, away, lambda copy: copy.start())

            for kind in range(3):
                f_x_start(kind, 0)
                f_c(kind, 0, 0).start()
        if index >= 2:
            from_x(index - 2)
            from_y(index - 2)
    for index in (z_size - 2, z_size - 1):
        from_x(index)
        from_y(index)

    def hand_on(kind, step):
        f_z_wait(kind, step)
        f_x_start(kind, step)
        f_c(kind, step, 0).start()

    def cross(kind, step):
        f_x_wait(kind, step)
        f_c(kind, step, 1).start()

    def pass_cotangent(step):
        d_z_in(order[step]).wait_recv()

        @pl.when(inner)
        def _():
            d_z(step).start()

        d_y(order[step]).start()

    def pass_if(case, step):
        @pl.when(case)
        def _():
            pass_cotangent(step)

    outer = first_z + last_z > 0
    tok_y_in.wait_recv()
    own_q.wait()
    own_o.wait()
    for kind in (0, 1):
        for step in range(z_size):
            for far in range(2):
                a_c_in(kind, step, far).wait_recv()

    gains = kv_w[:, 2 * head :].astype(jnp.float32).T[:8, :]
    gain_ref[...] = gains

    def norm_rows(index, carry):
        at = pl.ds(pl.multiple_of(index * 32, 32), 32)
        values = tok[at, :].astype(jnp.float32)
        scale = lax.rsqrt(jnp.mean(values * values, axis=-1, keepdims=True) + epsilon)
        n1_ref[at, :] = (values * scale * gain_ref[0:1, :]).astype(jnp.bfloat16)
        return carry

    lax.fori_loop(0, 2 * own // 32, norm_rows, 0)
    hand_on(0, order[1])
    table = (cos_ref[...], sin_ref[...])
    key_ref[...] = spin(dot_nn(n1_ref[...], kv_w[:, :head]), table).astype(jnp.bfloat16)
    val_ref[...] = dot_nn(n1_ref[...], kv_w[:, head : 2 * head]).astype(jnp.bfloat16)
    hand_on(0, order[2])
    head_scale = head ** (-0.5)
    heads = att_ref.shape[1] // head

    half_cols = att_ref.shape[1] // 2
    for index in range(2):
        cols = pl.ds(index * half_cols, half_cols)
        query[:, cols] = dot_nn(n1_ref[...], q_w[:, cols])

    def attend(index):
        cols = pl.ds(index * head, head)
        rotated = (spin(query[:, cols], table) * head_scale).astype(jnp.bfloat16)
        rot_ref[:, cols] = rotated
        probs = head_probs(rotated, key_ref[...], allow_ref[...]).astype(jnp.bfloat16)
        att_ref[:, cols] = dot_nn(probs, val_ref[...]).astype(jnp.bfloat16)

    tasks = [
        lambda: (pass_cotangent(1), pass_if(inner, 2)),
        lambda: hand_on(0, order[3]),
        lambda: (cross(0, 0), hand_on(1, order[1])),
        lambda: cross(1, 0),
        lambda: (cross(2, 0), hand_on(1, order[2])),
    ]
    for index in range(heads):
        attend(index)
        if index < len(tasks):
            tasks[index]()
    for step in range(z_size):
        for far in range(2):
            a_c_in(2, step, far).wait_recv()
    saves = [
        local(kv_w, kv_out),
        local(q_w, wq_out),
        local(o_w, wo_out),
    ]
    span = width // 4

    def project(index, carry):
        cols = pl.ds(pl.multiple_of(index * span, span), span)
        part[:, cols] = matmul_nt(att_ref[...], o_w[cols, :]).astype(jnp.bfloat16)
        return carry

    lax.fori_loop(0, 4, project, 0)
    part_out.start()
    hand_on(1, order[3])
    pass_if(outer, 2)
    pass_if(inner, 3)
    cross(0, order[1])
    hand_on(2, order[1])
    part_out.wait_recv()

    def middle(index, carry):
        at = pl.ds(pl.multiple_of(index * 32, 32), 32)
        there = pl.ds(pl.multiple_of(me_y * own + index * 32, 32), 32)
        values = (
            tok_ref[at, :].astype(jnp.float32)
            + part[there, :].astype(jnp.float32)
            + part_y[at, :].astype(jnp.float32)
        )
        mid_ref[at, :] = values
        scale = lax.rsqrt(jnp.mean(values * values, axis=-1, keepdims=True) + epsilon)
        n2_ref[there, :] = (values * scale * gain_ref[1:2, :]).astype(jnp.bfloat16)
        return carry

    lax.fori_loop(0, own // 32, middle, 0)
    n2_y.start()
    hand_on(2, order[2])
    cross(0, order[2])
    cross(0, order[3])
    hand_on(2, order[3])
    pass_if(outer, 3)
    for kind in (1, 2):
        for index in (1, 2, 3):
            cross(kind, order[index])
    for kind in range(3):
        for step in range(z_size):
            for far in range(2):
                f_c_in(kind, step, far).wait_recv()
    for step in range(z_size):
        d_y_in(step).wait_recv()
    n2_y_in.wait_recv()

    for kind in range(3):
        a_z_done(kind)
    d_z_done()
    tok_y.wait_send()
    part_out.wait_send()
    n2_y.wait_send()
    own_d.wait()
    for copy in saves:
        copy.wait()
    for step in range(z_size):
        d_y(step).wait_send()
        for far in range(2):
            kv_y(step, far).wait_send()
        for kind in range(3):
            if step:
                f_z(kind, step, lambda copy: copy.wait_send())
            a_x(kind, step).wait_send()
            f_x_done(kind, step)
            for far in range(2):
                a_c(kind, step, far).wait_send()
                f_c(kind, step, far).wait_send()


def pre_call(
    tokens, w_kv, gain_one, gain_two, table, segments, cotangent, w_query, w_out, ffn
):
    z_size = lax.axis_size("z")
    own, width = tokens.shape
    seq = 2 * own
    rows, cols = w_query.shape
    head = table[0].shape[1] * 2
    units = ragged_split(ffn[0].shape[1], z_size)[1]
    low = lambda *dims: jax.ShapeDtypeStruct(dims, jnp.bfloat16)
    full = lambda *dims: jax.ShapeDtypeStruct(dims, jnp.float32)
    dma = lambda *lead: pltpu.SemaphoreType.DMA(lead)
    vmem = pl.BlockSpec(memory_space=pltpu.VMEM)
    hbm = pl.BlockSpec(memory_space=pl.ANY)
    wide = lambda *lead: pltpu.VMEM((*lead, width), jnp.bfloat16)
    return pl.pallas_call(
        functools.partial(pre_kernel, z_size),
        out_shape=(
            low(seq, width),
            low(seq, cols),
            low(seq, head),
            low(seq, head),
            low(seq, cols),
            full(own, width),
            low(seq, width),
            full(8, width),
            full(seq, seq),
            low(width, 2 * head + 128),
            low(width, cols),
            low(width, cols),
            low(3, width, units),
            low(z_size, seq, width),
        ),
        in_specs=[vmem] * 7 + [hbm] * 6,
        out_specs=(vmem,) * 9 + (hbm,) * 5,
        scratch_shapes=[
            pltpu.VMEM((width, 2 * head + 128), jnp.bfloat16),
            pltpu.VMEM((width, cols), jnp.bfloat16),
            pltpu.VMEM((width, cols), jnp.bfloat16),
            wide(seq),
            wide(seq),
            wide(own),
            pltpu.VMEM((seq, cols), jnp.float32),
            pltpu.VMEM((128, 128), jnp.float32),
            dma(4),
            dma(4),
            dma(2 * z_size),
            dma(2 * z_size),
            dma(3, z_size + 1),
            dma(3, z_size),
            dma(3, z_size),
            dma(3, z_size),
            dma(3, 2 * z_size),
            dma(3, 2 * z_size),
            dma(3, z_size, 2),
            dma(3, z_size, 2),
            dma(3, z_size),
            dma(3, z_size),
            dma(3, 2 * z_size),
            dma(3, 2 * z_size),
            dma(z_size + 1),
            dma(z_size),
            dma(z_size),
            dma(z_size),
            dma(16),
        ],
        compiler_params=pltpu.CompilerParams(
            collective_id=1, has_side_effects=True, vmem_limit_bytes=VMEM_BYTES
        ),
        cost_estimate=pl.CostEstimate(
            flops=8 * seq * width * cols,
            bytes_accessed=8 * width * (cols + units),
            transcendentals=seq * seq * cols // head,
        ),
    )(tokens, w_kv, gain_one, gain_two, *table, segments, cotangent, w_query, w_out, *ffn)


def post_kernel(
    z_size,
    main,
    tok_ref,
    gain_ref,
    gain_part_ref,
    n1_ref,
    rot_ref,
    key_ref,
    val_ref,
    att_ref,
    cos_ref,
    sin_ref,
    allow_ref,
    kv_hbm,
    wq_hbm,
    wo_hbm,
    mix_hbm,
    gmf_hbm,
    gmb_hbm,
    mid_hbm,
    sums_hbm,
    mixed_ref,
    tgrad_ref,
    gsum_ref,
    kvg_ref,
    qg_ref,
    og_ref,
    ffn_out,
    kv_w,
    q_w,
    o_w,
    o_part,
    gm,
    gm_f,
    gq,
    gkv,
    kv_sum,
    back_y,
    mix_y,
    mix_z,
    mix_s,
    o_c,
    o_x,
    o_z,
    q_c,
    q_x,
    q_z,
    kv_y,
    kv_c,
    kv_x,
    kv_z,
    gain_own,
    gain_in,
    ffn_in,
    ffn_own,
    load_sem,
    own_sem,
    fx_send,
    fx_recv,
    fz_send,
    fz_recv,
    y_send,
    y_recv,
    my_send,
    my_recv,
    mz_send,
    mz_recv,
    wc_send,
    wc_recv,
    wx_send,
    wx_recv,
    wz_send,
    wz_recv,
    kc_send,
    kc_recv,
    kz_send,
    kz_recv,
    g_send,
    g_recv,
):
    me_z, me_x = lax.axis_index("z"), lax.axis_index("x")
    me_c, me_y = lax.axis_index("c"), lax.axis_index("mp")
    own, width = tok_ref.shape
    seq = 2 * own
    head = key_ref.shape[1]
    cols_here = att_ref.shape[1]
    heads = cols_here // head
    rows = qg_ref.shape[0]
    span = width // z_size
    mine = pl.ds(pl.multiple_of(me_y * own, own), own)
    theirs = pl.ds(pl.multiple_of((1 - me_y) * own, own), own)
    to_y, to_x, to_c = {"mp": 1 - me_y}, {"x": 1 - me_x}, {"c": 1 - me_c}
    head_scale = head ** (-0.5)

    def behind(step):
        return lax.rem(me_z - step + z_size, z_size)

    def to_z(step):
        return {"z": lax.rem(me_z + step, z_size)}

    def row_block(step, x_at, c_at):
        start = ((behind(step) * 2 + x_at) * 2 + c_at) * rows
        return pl.ds(pl.multiple_of(start, rows), rows)

    loads = [
        pltpu.make_async_copy(wo_hbm, o_w, load_sem.at[0]),
        pltpu.make_async_copy(wq_hbm, q_w, load_sem.at[1]),
        pltpu.make_async_copy(
            kv_hbm.at[:, :, :, :, :, pl.ds(0, 2 * head)], kv_w, load_sem.at[2]
        ),
    ]
    for step in range(z_size):
        loads.append(
            pltpu.make_async_copy(mix_hbm.at[step, me_y], mix_s.at[step], load_sem.at[3 + step])
        )
    loads.append(pltpu.make_async_copy(gmf_hbm, gm_f, load_sem.at[3 + z_size]))
    loads.append(pltpu.make_async_copy(gmb_hbm, gm.at[mine], load_sem.at[4 + z_size]))
    mid_load = pltpu.make_async_copy(mid_hbm, gm_f, load_sem.at[5 + z_size])
    for load in loads:
        load.start()

    barrier = pltpu.get_barrier_semaphore()
    peers = [to_y, to_x, to_c] + [to_z(step) for step in range(1, z_size)]
    for where in peers:
        pl.semaphore_signal(barrier, inc=1, device_id=where, device_id_type=MESH_ID)
    pl.semaphore_wait(barrier, len(peers))

    tasks = [(step, kind) for step in (2, 3) for kind in range(3)]

    def f_x(index):
        step, kind = tasks[index]
        return remote(
            sums_hbm.at[kind, step, 1],
            ffn_in.at[index],
            fx_send.at[index],
            fx_recv.at[index],
            to_x,
        )

    def f_own(index):
        step, kind = tasks[index]
        return pltpu.make_async_copy(
            sums_hbm.at[kind, step, 0], ffn_own.at[index % 2], own_sem.at[index % 2]
        )

    def f_z(step, kind, source_z, act):
        for case, columns in (
            ((source_z > 0) & (source_z < z_size - 1), ffn_out.shape[3]),
            ((source_z == 0) | (source_z == z_size - 1), main),
        ):

            @pl.when(case)
            def _(columns=columns):
                cols = pl.ds(0, columns)
                if step == 1:
                    src = sums_hbm.at[kind, 1, 0, :, cols]
                else:
                    src = ffn_in.at[tasks.index((step, kind)), :, cols]
                act(
                    remote(
                        src,
                        ffn_out.at[kind, step, :, cols],
                        fz_send.at[kind, step],
                        fz_recv.at[kind, step],
                        to_z(step),
                    )
                )

    def tick(index):
        step, kind = tasks[index]
        f_x(index).wait_recv()
        f_own(index).wait()
        block = ffn_in.at[index]
        add_rows(block, [ffn_own.at[index % 2]], block, rows)
        if index + 2 < len(tasks):
            f_own(index + 2).start()
        f_z(step, kind, me_z, lambda copy: copy.start())

    def f_x_own(kind):
        return remote(
            sums_hbm.at[kind, 0, 1],
            ffn_out.at[kind, 0],
            fx_send.at[len(tasks) + kind],
            fx_recv.at[len(tasks) + kind],
            to_x,
        )

    f_own(0).start()
    f_own(1).start()
    for index in range(len(tasks)):
        f_x(index).start()
    for kind in range(3):
        f_z(1, kind, me_z, lambda copy: copy.start())

    gm_y = remote(gmb_hbm, gm.at[mine], y_send.at[0], y_recv.at[0], to_y)
    gm_y_in = remote(gm.at[theirs], gm.at[theirs], y_send.at[0], y_recv.at[0], to_y)
    gm_y.start()

    first_z, last_z = (z_size - 1 - me_z) // (z_size - 1), me_z // (z_size - 1)
    inner = first_z + last_z == 0
    order = (
        0,
        1 + (me_z + 1) // 2,
        2 + (2 * me_z - 3) * (1 - first_z - last_z),
        3 - 2 * (me_z // 2),
    )
    right = (None, 1 - me_z // 2, (3 - me_z) * (2 - me_z) // 6 + me_z // 2 * (1 - last_z), 1 - me_z // 2)

    def hop_slot(index):
        step, way = order[index], right[index]
        return way * lax.rem(step + 1, z_size) + (1 - way) * (step - 1 + 4 * ((3 - step) // 2))

    def hop_target(index):
        return {"z": me_z + 2 * right[index] - 1}

    def mix_over_y(step):
        return remote(
            mix_hbm.at[step, 1 - me_y], mix_y.at[step], my_send.at[step], my_recv.at[step], to_y
        )

    def mix_over_z(index):
        slot = hop_slot(index)
        return remote(
            mix_s.at[order[index]],
            mix_z.at[slot],
            mz_send.at[index],
            mz_recv.at[slot],
            hop_target(index),
        )

    def mix_z_in(slot):
        return remote(mix_z.at[slot], mix_z.at[slot], mz_send.at[1], mz_recv.at[slot], to_z(1))

    def mix_add(step, others, last):
        def add_tile(tile, carry):
            at = pl.ds(pl.multiple_of(tile * TILE, TILE), TILE)
            total = mix_s[step, at, :].astype(jnp.float32)
            for other in others:
                total = total + other[at, :].astype(jnp.float32)
            if last:
                mixed_ref[:, at] = (gm_f[:, at] + total.T).astype(jnp.bfloat16)
            else:
                mix_s[step, at, :] = total.astype(jnp.bfloat16)
            return carry

        lax.fori_loop(0, width // TILE, add_tile, 0)

    def mix_step(index):
        step = order[index]
        mix_over_y(step).wait_recv()
        from_y = mix_y.at[step]
        if index:

            @pl.when(inner)
            def _():
                mix_z_in(step).wait_recv()
                mix_add(step, [from_y, mix_z.at[step]], False)

            @pl.when(first_z + last_z > 0)
            def _():
                mix_add(step, [from_y], False)

            mix_over_z(index).start()
        else:
            mid_load.wait()

            @pl.when(first_z == 0)
            def _():
                mix_z_in(0).wait_recv()

            @pl.when(last_z == 0)
            def _():
                mix_z_in(z_size).wait_recv()

            @pl.when(inner)
            def _():
                mix_add(0, [from_y, mix_z.at[0], mix_z.at[z_size]], True)

            @pl.when(first_z > 0)
            def _():
                mix_add(0, [from_y, mix_z.at[z_size]], True)

            @pl.when(last_z > 0)
            def _():
                mix_add(0, [from_y, mix_z.at[0]], True)

    for index in (1, 2, 3, 0):
        mix_over_y(order[index]).start()

    kinds = ((o_part, o_c, o_x, o_z, og_ref), (o_w, q_c, q_x, q_z, qg_ref))

    def w_c(kind, step, far):
        x_at = 1 - me_x if far else me_x
        return remote(
            kinds[kind][0].at[row_block(step, x_at, 1 - me_c)],
            kinds[kind][1].at[step, far],
            wc_send.at[kind, step, far],
            wc_recv.at[kind, step, far],
            to_c,
        )

    def w_x(kind, step):
        return remote(
            kinds[kind][0].at[row_block(step, 1 - me_x, me_c)],
            kinds[kind][2].at[step],
            wx_send.at[kind, step],
            wx_recv.at[kind, step],
            to_x,
        )

    def w_z(kind, index):
        step, slot = order[index], hop_slot(index)
        return remote(
            kinds[kind][0].at[row_block(step, me_x, me_c)],
            kinds[kind][3].at[slot],
            wz_send.at[kind, index],
            wz_recv.at[kind, slot],
            hop_target(index),
        )

    def w_z_in(kind, slot):
        block = kinds[kind][3].at[slot]
        return remote(block, block, wz_send.at[kind, 1], wz_recv.at[kind, slot], to_z(1))

    def w_x_stage(kind, index):
        step = order[index]
        w_c(kind, step, 1).wait_recv()
        block = kinds[kind][0].at[row_block(step, 1 - me_x, me_c)]
        add_rows(block, [kinds[kind][1].at[step, 1]], block, rows)
        w_x(kind, step).start()

    def w_z_stage(kind, index):
        part, from_c, from_x, from_z, result = kinds[kind]
        step = order[index]
        w_c(kind, step, 0).wait_recv()
        w_x(kind, step).wait_recv()
        block = part.at[row_block(step, me_x, me_c)]
        others = [from_c.at[step, 0], from_x.at[step]]
        if index:

            @pl.when(inner)
            def _():
                w_z_in(kind, step).wait_recv()
                add_rows(block, [*others, from_z.at[step]], block, rows)

            @pl.when(first_z + last_z > 0)
            def _():
                add_rows(block, others, block, rows)

            w_z(kind, index).start()
        else:

            @pl.when(first_z == 0)
            def _():
                w_z_in(kind, 0).wait_recv()

            @pl.when(last_z == 0)
            def _():
                w_z_in(kind, z_size).wait_recv()

            @pl.when(inner)
            def _():
                add_rows(block, [*others, from_z.at[0], from_z.at[z_size]], result, rows)

            @pl.when(first_z > 0)
            def _():
                add_rows(block, [*others, from_z.at[z_size]], result, rows)

            @pl.when(last_z > 0)
            def _():
                add_rows(block, [*others, from_z.at[0]], result, rows)

    def w_product(kind, index, left, values):
        step = order[index]
        at = pl.ds(pl.multiple_of(behind(step) * span, 128), span)
        turned = left[:, at].T

        def tile_body(tile, carry):
            cols = pl.ds(pl.multiple_of(tile * TILE, TILE), TILE)
            kinds[kind][0][at, cols] = dot_nn(turned, values[:, cols]).astype(jnp.bfloat16)
            return carry

        lax.fori_loop(0, cols_here // TILE, tile_body, 0)
        for far in (1, 0):
            w_c(kind, step, far).start()

    tick(0)
    tick(1)
    loads[-1].wait()
    gm_y_in.wait_recv()
    w_product(0, 1, gm, att_ref)
    w_product(0, 2, gm, att_ref)
    w_x_stage(0, 1)
    w_product(0, 3, gm, att_ref)
    w_x_stage(0, 2)
    tick(2)
    w_product(0, 0, gm, att_ref)
    w_x_stage(0, 3)
    for load in loads[:-1]:
        load.wait()

    kv_sum[...] = jnp.zeros(kv_sum.shape, jnp.float32)
    table = (cos_ref[...], sin_ref[...])

    for index in range(2):
        cols = pl.ds(index * (cols_here // 2), cols_here // 2)
        gq[:, cols] = dot_nn(gm[...], o_w[:, cols]).astype(jnp.bfloat16)

    def attend_back(index):
        cols = pl.ds(index * head, head)
        grad_vals = gq[:, cols]
        rotated = rot_ref[:, cols]
        probs = head_probs(rotated, key_ref[...], allow_ref[...])
        grad_probs = matmul_nt(grad_vals, val_ref[...])
        delta = jnp.sum(probs * grad_probs, axis=-1, keepdims=True)
        grad_scores = (probs * (grad_probs - delta)).astype(jnp.bfloat16)
        grad_rot = dot_nn(grad_scores, key_ref[...])
        gq[:, cols] = (spin_back(grad_rot, table) * head_scale).astype(jnp.bfloat16)
        kv_sum[0] += matmul_tn(grad_scores, rotated)
        kv_sum[1] += matmul_tn(probs.astype(jnp.bfloat16), grad_vals)

    for index in range(heads):
        attend_back(index)
        if index == 0:
            w_x_stage(0, 0)
        if 3 + index < len(tasks):
            tick(3 + index)
        if index == heads - 1:
            mix_step(1)
    gkv[:, :head] = spin_back(kv_sum[0], table).astype(jnp.bfloat16)
    gkv[:, head:] = kv_sum[1].astype(jnp.bfloat16)

    w_product(1, 1, n1_ref, gq)
    w_product(1, 2, n1_ref, gq)
    w_x_stage(1, 1)
    w_z_stage(0, 1)
    w_product(1, 3, n1_ref, gq)
    w_x_stage(1, 2)
    w_product(1, 0, n1_ref, gq)
    w_x_stage(1, 3)
    w_x_stage(1, 0)
    for kind in range(3):
        f_x_own(kind).start()

    gm_y.wait_send()
    back = gm
    def input_tile(index, carry):
        at = pl.ds(pl.multiple_of(index * span, 128), span)
        back[:, at] = (
            matmul_nt(gq[...], q_w[at, :]) + matmul_nt(gkv[...], kv_w[index].reshape(span, 2 * head))
        ).astype(jnp.bfloat16)
        return carry

    lax.fori_loop(0, z_size, input_tile, 0)
    back_out = remote(back.at[theirs], back_y, y_send.at[1], y_recv.at[1], to_y)
    back_out.start()

    kv_part = kv_w

    def kv_tile(index, carry):
        at = pl.ds(pl.multiple_of(index * span, 128), span)
        product = dot_nn(n1_ref[:, at].T, gkv[...]).astype(jnp.bfloat16)
        kv_part[index] = product.reshape(kv_part.shape[1:])
        return carry

    lax.fori_loop(0, z_size, kv_tile, 0)
    kv_over_y = remote(kv_part.at[:, :, :, 1 - me_y], kv_y, y_send.at[2], y_recv.at[2], to_y)
    kv_over_y.start()
    mix_step(2)
    w_z_stage(0, 2)
    mix_step(3)
    w_z_stage(0, 3)

    back_out.wait_recv()

    def input_rows(index, total):
        at = pl.ds(pl.multiple_of(index * 32, 32), 32)
        there = pl.ds(pl.multiple_of(me_y * own + index * 32, 32), 32)
        upstream = back[there, :].astype(jnp.float32) + back_y[at, :].astype(jnp.float32)
        grad, gain_part = norm_back(
            tok_ref[at, :].astype(jnp.float32), gain_ref[0:1, :], upstream
        )
        tgrad_ref[at, :] = (gm_f[at, :] + grad).astype(jnp.bfloat16)
        return total + gain_part

    attn_gain_part = lax.fori_loop(
        0, own // 32, input_rows, jnp.zeros((1, width), jnp.float32)
    )
    for index in range(4):
        at = slice(index * span, (index + 1) * span)
        gain_own[0, index : index + 1, :] = attn_gain_part[:, at]
        gain_own[0, 4 + index : 5 + index, :] = gain_part_ref[4 + index : 5 + index, :]

    def gain_send(stage, where):
        return remote(
            gain_own.at[stage], gain_in.at[stage], g_send.at[stage], g_recv.at[stage], where
        )

    gain_hops = [gain_send(0, to_y), gain_send(1, to_c), gain_send(2, to_x)]
    gain_last = [
        remote(
            gain_own.at[3], gain_in.at[2 + step], g_send.at[2 + step], g_recv.at[2 + step], to_z(step)
        )
        for step in range(1, z_size)
    ]

    def gain_fold(stage):
        gain_hops[stage].wait_recv()
        gain_own[stage + 1] = gain_own[stage] + gain_in[stage]

    gain_hops[0].start()
    mid_load.start()
    w_z_stage(1, 1)
    w_z_stage(0, 0)
    w_z_stage(1, 2)
    gain_fold(0)
    gain_hops[1].start()
    mix_step(0)
    w_z_stage(1, 3)
    gain_fold(1)
    gain_hops[2].start()
    kv_over_y.wait_recv()

    def kv_add_y(index, carry):
        for x_at in range(2):
            for c_at in range(2):
                block = kv_part.at[index, x_at, c_at, me_y]
                block[...] = (
                    block[...].astype(jnp.float32) + kv_y[index, x_at, c_at].astype(jnp.float32)
                ).astype(jnp.bfloat16)
        return carry

    lax.fori_loop(0, z_size, kv_add_y, 0)
    kv_over_c = remote(
        kv_part.at[:, :, 1 - me_c, me_y], kv_c, kc_send.at[0], kc_recv.at[0], to_c
    )
    kv_over_c.start()
    gain_fold(2)
    for copy in gain_last:
        copy.start()
    kv_over_c.wait_recv()

    def kv_add_c(index, carry):
        for x_at in range(2):
            block = kv_part.at[index, x_at, me_c, me_y]
            block[...] = (
                block[...].astype(jnp.float32) + kv_c[index, x_at].astype(jnp.float32)
            ).astype(jnp.bfloat16)
        return carry

    lax.fori_loop(0, z_size, kv_add_c, 0)
    kv_over_x = remote(
        kv_part.at[:, 1 - me_x, me_c, me_y], kv_x, kc_send.at[1], kc_recv.at[1], to_x
    )
    kv_over_x.start()
    w_z_stage(1, 0)
    kv_over_x.wait_recv()

    def kv_add_x(index, carry):
        block = kv_part.at[index, me_x, me_c, me_y]
        block[...] = (
            block[...].astype(jnp.float32) + kv_x[index].astype(jnp.float32)
        ).astype(jnp.bfloat16)
        return carry

    lax.fori_loop(0, z_size, kv_add_x, 0)
    kv_over_z = [
        remote(
            kv_part.at[lax.rem(me_z + step, z_size), me_x, me_c, me_y],
            kv_z.at[step - 1],
            kz_send.at[step],
            kz_recv.at[step],
            to_z(step),
        )
        for step in range(1, z_size)
    ]
    for copy in kv_over_z:
        copy.start()
    for copy in gain_last:
        copy.wait_recv()
    gsum_ref[...] = gain_own[3] + gain_in[3] + gain_in[4] + gain_in[5]
    for copy in kv_over_z:
        copy.wait_recv()
    kvg_ref[...] = (
        kv_part[me_z, me_x, me_c, me_y].astype(jnp.float32)
        + kv_z[0].astype(jnp.float32)
        + kv_z[1].astype(jnp.float32)
        + kv_z[2].astype(jnp.float32)
    )

    back_out.wait_send()
    kv_over_y.wait_send()
    kv_over_c.wait_send()
    kv_over_x.wait_send()
    for kind in range(3):
        f_x_own(kind).wait()
    for index in range(len(tasks)):
        f_x(index).wait_send()
    for step in range(1, z_size):
        for kind in range(3):
            f_z(step, kind, me_z, lambda copy: copy.wait_send())
            f_z(step, kind, behind(step), lambda copy: copy.wait_recv())
    for copy in gain_hops + gain_last + kv_over_z:
        copy.wait_send()
    for step in range(z_size):
        mix_over_y(step).wait_send()
        if step:
            mix_over_z(step).wait_send()
        for kind in range(2):
            w_c(kind, step, 0).wait_send()
            w_c(kind, step, 1).wait_send()
            w_x(kind, step).wait_send()
            if step:
                w_z(kind, step).wait_send()


def post_call(
    tokens,
    gains,
    gain_part,
    normed_one,
    rotated,
    keys,
    values,
    attn_vals,
    table,
    allowed,
    kv_weight,
    query_weight,
    out_weight,
    mix_parts,
    grad_mid,
    grad_mid_low,
    mid,
    ffn_sums,
    main,
):
    z_size = lax.axis_size("z")
    own, width = tokens.shape
    seq = 2 * own
    head = keys.shape[1]
    cols = attn_vals.shape[1]
    rows = width // (4 * z_size)
    units = ffn_sums.shape[4]
    low = lambda *dims: pltpu.VMEM(dims, jnp.bfloat16)
    full = lambda *dims: pltpu.VMEM(dims, jnp.float32)
    out_full = lambda *dims: jax.ShapeDtypeStruct(dims, jnp.float32)
    out_low = lambda *dims: jax.ShapeDtypeStruct(dims, jnp.bfloat16)
    dma = lambda *lead: pltpu.SemaphoreType.DMA(lead)
    vmem = pl.BlockSpec(memory_space=pltpu.VMEM)
    hbm = pl.BlockSpec(memory_space=pl.ANY)
    z = z_size
    return pl.pallas_call(
        functools.partial(post_kernel, z_size, main),
        out_shape=(
            out_low(own, width),
            out_low(own, width),
            out_full(8, width // z),
            out_full(rows // 2, 2 * head),
            out_full(rows, cols),
            out_full(rows, cols),
            out_low(3, z, rows, units),
        ),
        in_specs=[vmem] * 11 + [hbm] * 8,
        out_specs=(vmem,) * 6 + (hbm,),
        scratch_shapes=[
            low(z, 2, 2, 2, rows // 2, 2 * head),
            low(width, cols),
            low(width, cols),
            low(width, cols),
            low(seq, width),
            full(own, width),
            low(seq, cols),
            low(seq, 2 * head),
            full(2, seq, head),
            low(own, width),
            low(z, width, own),
            low(z + 1, width, own),
            low(z, width, own),
            low(z, 2, rows, cols),
            low(z, rows, cols),
            low(z + 1, rows, cols),
            low(z, 2, rows, cols),
            low(z, rows, cols),
            low(z + 1, rows, cols),
            low(z, 2, 2, rows // 2, 2 * head),
            low(z, 2, rows // 2, 2 * head),
            low(z, rows // 2, 2 * head),
            low(z - 1, rows // 2, 2 * head),
            full(4, 8, width // z),
            full(6, 8, width // z),
            low(6, rows, units),
            low(2, rows, units),
            dma(6 + z),
            dma(2),
            dma(9),
            dma(9),
            dma(3, z),
            dma(3, z),
            dma(3),
            dma(3),
            dma(z),
            dma(z),
            dma(z),
            dma(z + 1),
            dma(2, z, 2),
            dma(2, z, 2),
            dma(2, z),
            dma(2, z),
            dma(2, z),
            dma(2, z + 1),
            dma(2),
            dma(2),
            dma(z),
            dma(z),
            dma(6),
            dma(6),
        ],
        compiler_params=pltpu.CompilerParams(
            collective_id=2, has_side_effects=True, vmem_limit_bytes=VMEM_BYTES
        ),
        cost_estimate=pl.CostEstimate(
            flops=14 * seq * width * cols,
            bytes_accessed=10 * width * cols,
            transcendentals=seq * seq * cols // head,
        ),
    )(
        tokens,
        gains,
        gain_part,
        normed_one,
        rotated,
        keys,
        values,
        attn_vals,
        *table,
        allowed,
        kv_weight.reshape(z, 2, 2, 2, rows // 2, kv_weight.shape[1]),
        query_weight,
        out_weight,
        mix_parts,
        grad_mid,
        grad_mid_low,
        mid,
        ffn_sums,
    )


def layout_kernel(
    z_size,
    main,
    sum_ref,
    ffn_ref,
    q_ref,
    o_ref,
    kv_ref,
    mixed_in,
    tgrad_in,
    wg_ref,
    wu_ref,
    wd_ref,
    qg_ref,
    og_ref,
    kvg_ref,
    mixed_ref,
    tgrad_ref,
):
    me_z = lax.axis_index("z")
    for kind, out in enumerate((wg_ref, wu_ref, wd_ref)):
        for step in range(z_size):
            at = lax.rem(me_z - step + z_size, z_size)
            values = ffn_ref[kind, step].astype(jnp.float32)
            if step == 0:
                values = values + sum_ref[kind, 0, 0].astype(jnp.float32)
            body = pl.ds(pl.multiple_of(at * main, 128), main)
            out[:, body] = values[:, :main]

            @pl.when((at > 0) & (at < z_size - 1))
            def _(out=out, at=at, values=values):
                tail = z_size * main + lax.rem(at + 1, 2) * 128
                out[:, pl.ds(pl.multiple_of(tail, 128), 128)] = values[:, main:]
    qg_ref[...] = q_ref[...]
    og_ref[...] = o_ref[...]
    kvg_ref[...] = kv_ref[...]
    mixed_ref[...] = mixed_in[...]
    tgrad_ref[...] = tgrad_in[...]


def layout_call(ffn_sums, ffn_grads, query_grad, out_grad, kv_grad, mixed, tokens_grad, ffn_cols):
    z_size = lax.axis_size("z")
    main, units = ragged_split(ffn_cols, z_size)
    rows, cols = query_grad.shape
    parts = rows // 80
    kv_rows = kv_grad.shape[0] // parts
    full = lambda *dims: jax.ShapeDtypeStruct(dims, jnp.float32)
    row = lambda height, width: pl.BlockSpec((height, width), lambda index: (index, 0))
    own, width = mixed.shape
    share = pl.BlockSpec((own, width // parts), lambda index: (0, index))
    specs = [row(80, cols), row(80, cols), row(kv_rows, kv_grad.shape[1]), share, share]
    return pl.pallas_call(
        functools.partial(layout_kernel, z_size, main),
        grid=(parts,),
        out_shape=(
            *[full(rows, ffn_cols)] * 3,
            full(rows, cols),
            full(rows, cols),
            full(*kv_grad.shape),
            jax.ShapeDtypeStruct(mixed.shape, jnp.bfloat16),
            jax.ShapeDtypeStruct(mixed.shape, jnp.bfloat16),
        ),
        in_specs=[
            pl.BlockSpec((3, 1, 1, 80, units), lambda index: (0, 0, 0, index, 0)),
            pl.BlockSpec((3, z_size, 80, units), lambda index: (0, 0, index, 0)),
            *specs,
        ],
        out_specs=(*[row(80, ffn_cols)] * 3, *specs),
        compiler_params=pltpu.CompilerParams(vmem_limit_bytes=VMEM_BYTES),
    )(ffn_sums, ffn_grads, query_grad, out_grad, kv_grad, mixed, tokens_grad)


FF_SPLIT = 4


def ffn_pass(normed, grad_out, gate_weight, up_weight, down_weight):
    gate = jnp.dot(normed, gate_weight, preferred_element_type=jnp.float32)
    up_proj = jnp.dot(normed, up_weight, preferred_element_type=jnp.float32)
    grad_hidden = jnp.dot(grad_out, down_weight, preferred_element_type=jnp.float32)
    product, pull = jax.vjp(gelu_product, gate, up_proj)
    hidden = product.astype(jnp.bfloat16)
    grad_gate_f, grad_up_f = pull(grad_hidden)
    grad_gate = grad_gate_f.astype(jnp.bfloat16)
    grad_up = grad_up_f.astype(jnp.bfloat16)
    mixed_part = matmul_nt(hidden, down_weight).astype(jnp.bfloat16)
    normed_part = (matmul_nt(grad_gate, gate_weight) + matmul_nt(grad_up, up_weight)).astype(
        jnp.bfloat16
    )
    weight_parts = [
        matmul_tn(normed, grad_gate).astype(jnp.bfloat16),
        matmul_tn(normed, grad_up).astype(jnp.bfloat16),
        matmul_tn(grad_out, hidden).astype(jnp.bfloat16),
    ]
    return mixed_part, normed_part, weight_parts


def shards_general(
    tokens,
    segments,
    positions,
    cotangent,
    attn_gain,
    ffn_gain,
    w_kv,
    w_query,
    w_out,
    w_gate,
    w_up,
    w_down,
):
    everywhere = ("z", "xc", "mp")
    dp = ("z", "xc")
    z_size = lax.axis_size("z")
    xc_size = lax.axis_size("xc")
    gains = lax.all_gather(
        jnp.stack([attn_gain, ffn_gain], axis=1), everywhere, axis=0, tiled=True
    ).astype(jnp.float32)
    gain_one, gain_two = gains[:, 0], gains[:, 1]
    kv_weight = lax.all_gather(w_kv, everywhere, axis=0, tiled=True)
    head_dim = kv_weight.shape[1] // 2
    width = tokens.shape[1]
    seq_len = segments.shape[0]
    heads_here = w_query.shape[1] // head_dim
    scale = head_dim ** (-0.5)
    cosine, sine = rotary_angles(positions, head_dim)
    inputs_f = tokens.astype(jnp.float32)
    tokens_all = lax.all_gather(tokens, "mp", axis=0, tiled=True)
    normed_one = norm_gain(tokens_all.astype(jnp.float32), gain_one).astype(jnp.bfloat16)
    query_weight = lax.all_gather(w_query, dp, axis=0, tiled=True)
    out_weight = lax.all_gather(w_out, dp, axis=0, tiled=True)

    rows = w_gate.shape[0]
    unit = w_gate.shape[1] // z_size

    def spread(weight):
        pieces = weight.reshape(rows, z_size, unit).transpose(1, 0, 2)
        pieces = lax.all_to_all(pieces, "z", split_axis=0, concat_axis=0, tiled=True)
        return lax.all_gather(pieces, "xc", axis=1, tiled=False).reshape(width, unit)

    gate_weight, up_weight, down_weight = spread(w_gate), spread(w_up), spread(w_down)
    grad_all = lax.all_gather(cotangent, ("z", "mp"), axis=0, tiled=True)

    query = jnp.dot(normed_one, query_weight, preferred_element_type=jnp.float32).reshape(
        seq_len, heads_here, head_dim
    )
    rotated = (rotate(query, cosine[:, None], sine[:, None]) * scale).astype(jnp.bfloat16)
    keyval = jnp.dot(normed_one, kv_weight, preferred_element_type=jnp.float32)
    keys = rotate(keyval[:, :head_dim], cosine, sine).astype(jnp.bfloat16)
    values = keyval[:, head_dim:].astype(jnp.bfloat16)
    allowed = block_allowed(segments, 0, seq_len)
    scores = jnp.einsum("thd,sd->hts", rotated, keys, preferred_element_type=jnp.float32)
    scores = jnp.where(allowed[None], scores, masked_score)
    row_max = jnp.max(scores, axis=-1, keepdims=True)
    weights = jnp.exp(scores - row_max)
    probs = weights / jnp.sum(weights, axis=-1, keepdims=True)
    probs_low = probs.astype(jnp.bfloat16)
    attn_vals = (
        jnp.einsum("hts,sd->thd", probs_low, values, preferred_element_type=jnp.float32)
        .reshape(seq_len, heads_here * head_dim)
        .astype(jnp.bfloat16)
    )
    mid = inputs_f + lax.psum_scatter(
        matmul_nt(attn_vals, out_weight).astype(jnp.bfloat16),
        "mp",
        scatter_dimension=0,
        tiled=True,
    ).astype(jnp.float32)
    normed_two = norm_gain(mid, gain_two).astype(jnp.bfloat16)
    normed_all = lax.all_gather(normed_two, ("z", "mp"), axis=0, tiled=True)

    mixed_part, normed_part, weight_parts = ffn_pass(
        normed_all, grad_all, gate_weight, up_weight, down_weight
    )
    grad_normed_two = lax.psum_scatter(
        normed_part, ("z", "mp"), scatter_dimension=0, tiled=True
    ).astype(jnp.float32)
    mixed = (
        mid
        + lax.psum_scatter(mixed_part, ("z", "mp"), scatter_dimension=0, tiled=True).astype(
            jnp.float32
        )
    ).astype(jnp.bfloat16)

    def collect(part):
        pieces = part.reshape(z_size, xc_size, rows, unit).transpose(1, 0, 2, 3)
        pieces = pieces.reshape(xc_size * z_size * rows, unit)
        pieces = lax.psum_scatter(pieces, "xc", scatter_dimension=0, tiled=True)
        pieces = pieces.reshape(z_size, rows, unit)
        pieces = lax.all_to_all(pieces, "z", split_axis=0, concat_axis=0, tiled=True)
        return pieces.transpose(1, 0, 2).reshape(rows, z_size * unit).astype(jnp.float32)

    w_gate_grad, w_up_grad, w_down_grad = [collect(part) for part in weight_parts]

    norm_pull_two = jax.vjp(norm_gain, mid, gain_two)[1]
    grad_mid_norm, grad_gain_two = norm_pull_two(grad_normed_two)
    grad_mid = cotangent.astype(jnp.float32) + grad_mid_norm
    grad_mid_all = lax.all_gather(grad_mid.astype(jnp.bfloat16), "mp", axis=0, tiled=True)
    grad_vals = (
        jnp.dot(grad_mid_all, out_weight, preferred_element_type=jnp.float32)
        .astype(jnp.bfloat16)
        .reshape(seq_len, heads_here, head_dim)
    )
    grad_probs = jnp.einsum("thd,sd->hts", grad_vals, values, preferred_element_type=jnp.float32)
    delta = jnp.sum(probs * grad_probs, axis=-1, keepdims=True)
    grad_scores = (probs * (grad_probs - delta)).astype(jnp.bfloat16)
    grad_rot = jnp.einsum("hts,sd->thd", grad_scores, keys, preferred_element_type=jnp.float32)
    key_sum = jnp.einsum("hts,thd->sd", grad_scores, rotated, preferred_element_type=jnp.float32)
    value_sum = jnp.einsum("hts,thd->sd", probs_low, grad_vals, preferred_element_type=jnp.float32)
    grad_query = (
        (unrotate(grad_rot, cosine[:, None], sine[:, None]) * scale)
        .reshape(seq_len, heads_here * head_dim)
        .astype(jnp.bfloat16)
    )
    grad_kv = jnp.concatenate([unrotate(key_sum, cosine, sine), value_sum], axis=1).astype(
        jnp.bfloat16
    )
    grad_normed_one = lax.psum_scatter(
        (matmul_nt(grad_query, query_weight) + matmul_nt(grad_kv, kv_weight)).astype(jnp.bfloat16),
        "mp",
        scatter_dimension=0,
        tiled=True,
    ).astype(jnp.float32)
    norm_pull_one = jax.vjp(norm_gain, inputs_f, gain_one)[1]
    grad_input_norm, grad_gain_one = norm_pull_one(grad_normed_one)
    tokens_grad = (grad_mid + grad_input_norm).astype(jnp.bfloat16)

    w_query_grad = lax.psum_scatter(
        matmul_tn(normed_one, grad_query).astype(jnp.bfloat16), dp, scatter_dimension=0, tiled=True
    ).astype(jnp.float32)
    w_out_grad = lax.psum_scatter(
        matmul_tn(grad_mid_all, attn_vals).astype(jnp.bfloat16), dp, scatter_dimension=0, tiled=True
    ).astype(jnp.float32)
    small = jnp.concatenate(
        [matmul_tn(normed_one, grad_kv), grad_gain_one[:, None], grad_gain_two[:, None]], axis=1
    )
    small = lax.psum_scatter(small, everywhere, scatter_dimension=0, tiled=True)
    kv_grad = small[:, : 2 * head_dim]
    return (
        mixed,
        tokens_grad,
        small[:, 2 * head_dim],
        small[:, 2 * head_dim + 1],
        kv_grad,
        w_query_grad,
        w_out_grad,
        w_gate_grad,
        w_up_grad,
        w_down_grad,
    )


def shards_fast(
    tokens,
    segments,
    positions,
    cotangent,
    attn_gain,
    ffn_gain,
    w_kv,
    w_query,
    w_out,
    w_gate,
    w_up,
    w_down,
):
    quarter = w_kv.shape[1] // 8
    lane = jnp.arange(2 * quarter)
    freqs = rope_base ** (-(lane % quarter).astype(jnp.float32) / quarter)
    phase = positions.astype(jnp.float32)[:, None] * freqs[None, :]
    table = (jnp.cos(phase), jnp.where(lane < quarter, -1.0, 1.0)[None, :] * jnp.sin(phase))
    (
        normed_one,
        rotated,
        keys,
        values,
        attn_vals,
        mid,
        normed_two,
        gains,
        allowed,
        kv_weight,
        query_weight,
        out_weight,
        ffn_weights,
        grad_all,
    ) = pre_call(
        tokens,
        w_kv,
        attn_gain[None, :],
        ffn_gain[None, :],
        table,
        segments[None, :],
        cotangent,
        w_query,
        w_out,
        (w_gate, w_up, w_down),
    )
    main = ragged_split(w_gate.shape[1], lax.axis_size("z"))[0]
    grad_mid, gain_part, mix_parts, ffn_sums, grad_mid_low = ffn_call(
        gains, normed_two, grad_all, ffn_weights, mid, w_gate.shape[0], main
    )
    mixed, tokens_grad, gain_grads, kv_grad, query_grad, out_grad, ffn_grads = post_call(
        tokens,
        gains,
        gain_part,
        normed_one,
        rotated,
        keys,
        values,
        attn_vals,
        table,
        allowed,
        kv_weight,
        query_weight,
        out_weight,
        mix_parts,
        grad_mid,
        grad_mid_low,
        mid,
        ffn_sums,
        main,
    )
    *ffn_out, query_grad, out_grad, kv_grad, mixed, tokens_grad = layout_call(
        ffn_sums,
        ffn_grads,
        query_grad,
        out_grad,
        kv_grad,
        mixed,
        tokens_grad,
        w_gate.shape[1],
    )
    share = attn_gain.shape[0]
    place = lax.axis_index(("z", "x", "c", "mp")) * share
    gain_grads = gain_grads.reshape(2, gain_grads.size // 2)
    gain_grads = lax.dynamic_slice(gain_grads, (0, place), (2, share))
    return (
        mixed,
        tokens_grad,
        gain_grads[0],
        gain_grads[1],
        kv_grad,
        query_grad,
        out_grad,
        *ffn_out,
    )


def solution(mesh):
    dp_size, mp_size = mesh.shape["dp"], mesh.shape["mp"]
    if dp_size == 4 * FF_SPLIT and mp_size == 2:
        body, dp = shards_fast, ("z", "x", "c")
        sizes = (FF_SPLIT, 2, 2, mp_size)
    else:
        body, dp = shards_general, ("z", "xc")
        sizes = (FF_SPLIT, dp_size // FF_SPLIT, mp_size)
    all_axes = (*dp, "mp")
    fine = jax.sharding.Mesh(mesh.devices.reshape(sizes), all_axes)
    in_specs = (
        P(all_axes, None),
        P(dp),
        P(dp),
        P(all_axes, None),
        P(all_axes),
        P(all_axes),
        P(all_axes, None),
        P(dp, "mp"),
        P(dp, "mp"),
        P(dp, "mp"),
        P(dp, "mp"),
        P(dp, "mp"),
    )
    out_specs = (
        P(all_axes, None),
        P(all_axes, None),
        P(all_axes),
        P(all_axes),
        P(all_axes, None),
        P(dp, "mp"),
        P(dp, "mp"),
        P(dp, "mp"),
        P(dp, "mp"),
        P(dp, "mp"),
    )
    return jax.shard_map(body, mesh=fine, in_specs=in_specs, out_specs=out_specs, check_vma=False)
```

```python
import functools

import jax
import jax.numpy as jnp
from jax import lax
from jax.experimental import pallas as pl
from jax.experimental.pallas import tpu as pltpu
from jax.sharding import PartitionSpec as P

WINDOW = 2048


epsilon = 1e-06
rope_base = 10000.0
masked_score = -1e30
VMEM_BYTES = 66_000_000


def norm_gain(values, gain):
    return values * lax.rsqrt(jnp.mean(values * values, axis=-1, keepdims=True) + epsilon) * gain


def rotary_angles(positions, head_width):
    quarter = head_width // 4
    freqs = rope_base ** (-jnp.arange(quarter).astype(jnp.float32) / quarter)
    phase = positions.astype(jnp.float32)[:, None] * freqs[None, :]
    return (jnp.cos(phase), jnp.sin(phase))


def rotate(values, cosine, sine):
    quarter = cosine.shape[-1]
    first_half = values[..., :quarter]
    second_half = values[..., quarter : 2 * quarter]
    return jnp.concatenate(
        [
            first_half * cosine - second_half * sine,
            second_half * cosine + first_half * sine,
            values[..., 2 * quarter :],
        ],
        axis=-1,
    )


def unrotate(values, cosine, sine):
    quarter = cosine.shape[-1]
    first_half = values[..., :quarter]
    second_half = values[..., quarter : 2 * quarter]
    return jnp.concatenate(
        [
            first_half * cosine + second_half * sine,
            second_half * cosine - first_half * sine,
            values[..., 2 * quarter :],
        ],
        axis=-1,
    )


def gelu_product(gate, up_proj):
    return jax.nn.gelu(gate, approximate=True) * up_proj


def matmul_nt(left, right):
    return lax.dot_general(
        left, right, (((1,), (1,)), ((), ())), preferred_element_type=jnp.float32
    )


def matmul_tn(left, right):
    return lax.dot_general(
        left, right, (((0,), (0,)), ((), ())), preferred_element_type=jnp.float32
    )


def block_allowed(segments, first_row, rows):
    seq_len = segments.shape[0]
    query_rows = first_row + jnp.arange(rows)
    key_rows = jnp.arange(seq_len)
    return (
        (segments[:, None] == segments[None, :])
        & (key_rows[None, :] <= query_rows[:, None])
        & (query_rows[:, None] - key_rows[None, :] < WINDOW)
    )


MESH_ID = pl.DeviceIdType.MESH
GELU_A = 0.7978845608028654
GELU_B = 0.044715
TILE = 256
WIDE = 512


def remote(src, dst, send_sem, recv_sem, where):
    return pltpu.make_async_remote_copy(
        src_ref=src,
        dst_ref=dst,
        send_sem=send_sem,
        recv_sem=recv_sem,
        device_id=where,
        device_id_type=MESH_ID,
    )


class Halves:
    def __init__(self, src, dst, send_sem, recv_sem, where):
        rows = src.shape[0] // 2
        cuts = [pl.ds(part * rows, rows) for part in range(2)]
        self.copies = [
            remote(src.at[cut], dst.at[cut], send_sem.at[part], recv_sem.at[part], where)
            for part, cut in enumerate(cuts)
        ]

    def start(self):
        for copy in self.copies:
            copy.start()

    def wait_recv(self):
        for copy in self.copies:
            copy.wait_recv()

    def wait_send(self):
        for copy in self.copies:
            copy.wait_send()


def dot_nn(left, right):
    return lax.dot_general(
        left, right, (((1,), (0,)), ((), ())), preferred_element_type=jnp.float32
    )


def gelu_parts(gate):
    square = gate * gate
    bend = jnp.tanh(GELU_A * gate * (1.0 + GELU_B * square))
    half = 0.5 * (1.0 + bend)
    slope = half + 0.5 * gate * (1.0 - bend * bend) * GELU_A * (1.0 + 3.0 * GELU_B * square)
    return gate * half, slope


def add_rows(first, rest, out, count):
    def body(index, carry):
        step = pl.ds(pl.multiple_of(index * 32, 32), 32)
        total = first[step, :].astype(jnp.float32)
        for other in rest:
            total = total + other[step, :].astype(jnp.float32)
        out[step, :] = total.astype(out.dtype)
        return carry

    lax.fori_loop(0, count // 32, body, 0)


def norm_back(values, gain, upstream):
    scale = lax.rsqrt(jnp.mean(values * values, axis=-1, keepdims=True) + epsilon)
    normed = values * scale
    pulled = gain * upstream
    back = scale * (pulled - normed * jnp.mean(normed * pulled, axis=-1, keepdims=True))
    return back, jnp.sum(upstream * normed, axis=0, keepdims=True)


def ffn_kernel(
    z_size,
    main,
    gain_ref,
    own_hbm,
    dy_hbm,
    w_hbm,
    mid_hbm,
    gm_ref,
    gain_part,
    mix_hbm,
    sums_hbm,
    gm_hbm,
    n2,
    dy,
    w3,
    h3,
    n2_t,
    dy_t,
    gn_part,
    mix_buf,
    gn_y,
    gn_z,
    gn_s,
    c_in,
    x_in,
    mid,
    load_sem,
    mix_sem,
    ag_y_send,
    ag_y_recv,
    ag_z_send,
    ag_z_recv,
    rs_y_send,
    rs_y_recv,
    rs_z_send,
    rs_z_recv,
    c_send,
    c_recv,
    x_send,
    x_recv,
    out_sem,
):
    own = own_hbm.shape[0] // 2
    width = own_hbm.shape[1]
    units = w3.shape[2]
    rows = c_in.shape[3]
    span = width // z_size
    me_y, me_z = lax.axis_index("mp"), lax.axis_index("z")
    me_x, me_c = lax.axis_index("x"), lax.axis_index("c")
    mine = pl.ds(pl.multiple_of(me_y * own, own), own)
    theirs = pl.ds(pl.multiple_of((1 - me_y) * own, own), own)
    to_y, to_x, to_c = {"mp": 1 - me_y}, {"x": 1 - me_x}, {"c": 1 - me_c}

    def ahead(step):
        return lax.rem(me_z + step, z_size)

    def to_z(step):
        return {"z": ahead(step)}

    def row_block(z_at, x_at, c_at):
        return pl.ds(pl.multiple_of(((z_at * 2 + x_at) * 2 + c_at) * rows, rows), rows)

    inner = (me_z > 0) & (me_z < z_size - 1)
    outer = (me_z == 0) | (me_z == z_size - 1)

    def w_load(index, columns):
        cols = pl.ds(0, columns)
        return pltpu.make_async_copy(
            w_hbm.at[index, :, cols], w3.at[index, :, cols], load_sem.at[z_size + index]
        )

    def w_loads(act):
        for case, columns in ((inner, units), (outer, main)):

            @pl.when(case)
            def _(columns=columns):
                for index in range(3):
                    act(w_load(index, columns))

    w_loads(lambda copy: copy.start())
    dy_loads = [
        pltpu.make_async_copy(dy_hbm.at[index], dy, load_sem.at[index])
        for index in range(z_size)
    ]
    own_load = pltpu.make_async_copy(own_hbm, n2.at[0], load_sem.at[z_size + 3])
    mid_load = pltpu.make_async_copy(mid_hbm, mid, load_sem.at[z_size + 4])
    for load in (own_load, dy_loads[0], mid_load):
        load.start()

    barrier = pltpu.get_barrier_semaphore()
    peers = [to_y, to_x, to_c] + [to_z(step) for step in range(1, z_size)]
    for where in peers:
        pl.semaphore_signal(barrier, inc=1, device_id=where, device_id_type=MESH_ID)
    pl.semaphore_wait(barrier, len(peers))

    def ag_y(index):
        block = n2.at[index, mine]
        return Halves(block, block, ag_y_send.at[index], ag_y_recv.at[index], to_y)

    def ag_y_in(index):
        block = n2.at[index, theirs]
        return Halves(block, block, ag_y_send.at[index], ag_y_recv.at[index], to_y)

    def ag_z(index):
        src = own_hbm.at[mine] if index == 0 else n2.at[index, mine]
        return Halves(
            src, n2.at[index + 1, mine], ag_z_send.at[index], ag_z_recv.at[index + 1], to_z(1)
        )

    def ag_z_in(index):
        block = n2.at[index, mine]
        return Halves(block, block, ag_z_send.at[0], ag_z_recv.at[index], to_z(1))

    def ag_last():
        return Halves(
            n2.at[2, theirs], n2.at[3, theirs], ag_y_send.at[3], ag_y_recv.at[3], to_z(1)
        )

    def forward(index):
        ag_z_in(index).wait_recv()
        ag_z(index).start()
        ag_y(index).start()

    ag_z(0).start()

    mix_copies = []

    def turn(source, target, index):
        def turn_tile(tile, carry):
            at = pl.ds(pl.multiple_of(tile * span, 128), span)
            target[at, pl.ds(index * 2 * own, 2 * own)] = source[:, at].T
            return carry

        lax.fori_loop(0, z_size, turn_tile, 0)

    def chunk(index):
        if index:
            mix_copies[index - 1].wait()
        dy_loads[index].wait()
        rows_at = pl.ds(index * 2 * own, 2 * own)

        def up_tile(tile, carry):
            cols = pl.ds(pl.multiple_of(tile * WIDE, WIDE), WIDE)
            gate = dot_nn(n2[index], w3[0, :, cols])
            up_proj = dot_nn(n2[index], w3[1, :, cols])
            grad_hidden = dot_nn(dy[...], w3[2, :, cols])
            act, slope = gelu_parts(gate)
            h3[0, rows_at, cols] = (grad_hidden * up_proj * slope).astype(jnp.bfloat16)
            h3[1, rows_at, cols] = (grad_hidden * act).astype(jnp.bfloat16)
            h3[2, rows_at, cols] = (act * up_proj).astype(jnp.bfloat16)
            return carry

        lax.fori_loop(0, units // WIDE, up_tile, 0)

        def down_tile(tile, carry):
            at = pl.ds(pl.multiple_of(tile * span, 128), span)
            normed = matmul_nt(w3[0, at, :], h3[0, rows_at, :]) + matmul_nt(
                w3[1, at, :], h3[1, rows_at, :]
            )
            mixed = matmul_nt(w3[2, at, :], h3[2, rows_at, :])
            for half in range(2):
                cols = slice(half * own, (half + 1) * own)
                gn_part[index, half, at, :] = normed[:, cols].astype(jnp.bfloat16)
                mix_buf[half, at, :] = mixed[:, cols].astype(jnp.bfloat16)
            return carry

        lax.fori_loop(0, z_size, down_tile, 0)
        copy = pltpu.make_async_copy(mix_buf, mix_hbm.at[index], mix_sem.at[index])
        copy.start()
        mix_copies.append(copy)
        if index:
            rs_y(index).start()
        turn(n2.at[index], n2_t, index)
        turn(dy, dy_t, index)
        if index + 1 < z_size:
            dy_loads[index + 1].start()

    def rs_y(index):
        return Halves(
            gn_part.at[index, 1 - me_y], gn_y.at[index], rs_y_send.at[index], rs_y_recv.at[index], to_y
        )

    def rs_z(index):
        return Halves(
            gn_s.at[index - 1],
            gn_z.at[index - 1],
            rs_z_send.at[index],
            rs_z_recv.at[index - 1],
            to_z(1),
        )

    def rs_step(index):
        rs_y(index).wait_recv()
        slot = (index - 2) % z_size
        if index != 1:
            Halves(
                gn_s.at[slot], gn_z.at[slot], rs_z_send.at[1], rs_z_recv.at[slot], to_z(1)
            ).wait_recv()

        def add_tile(tile, carry):
            at = pl.ds(pl.multiple_of(tile * TILE, TILE), TILE)
            total = gn_part[index, me_y, at, :].astype(jnp.float32) + gn_y[index, at, :].astype(
                jnp.float32
            )
            if index != 1:
                total = total + gn_z[slot, at, :].astype(jnp.float32)
            if index == 0:
                gm_ref[:, at] = total.T
            else:
                gn_s[index - 1, at, :] = total.astype(jnp.bfloat16)
            return carry

        lax.fori_loop(0, width // TILE, add_tile, 0)
        if index != 0:
            rs_z(index).start()


    def grads(step):
        at = pl.ds(pl.multiple_of(ahead(step) * span, 128), span)
        for kind, source in enumerate((n2_t, n2_t, dy_t)):

            def tile_body(tile, carry, kind=kind, source=source):
                cols = pl.ds(pl.multiple_of(tile * WIDE, WIDE), WIDE)
                w3[kind, at, cols] = dot_nn(source[at, :], h3[kind, :, cols]).astype(jnp.bfloat16)
                return carry

            lax.fori_loop(0, units // WIDE, tile_body, 0)
            for far in (1, 0):
                over_c(kind, step, far).start()

    def over_c(kind, step, far):
        x_at = 1 - me_x if far else me_x
        return remote(
            w3.at[kind, row_block(ahead(step), x_at, 1 - me_c)],
            c_in.at[kind, step, far],
            c_send.at[kind, step, far],
            c_recv.at[kind, step, far],
            to_c,
        )

    def over_x(kind):
        return remote(
            w3.at[kind, row_block(ahead(1), 1 - me_x, me_c)],
            x_in.at[kind],
            x_send.at[kind],
            x_recv.at[kind],
            to_x,
        )

    out_copies = []

    def keep(kind, step, far, block):
        copy = pltpu.make_async_copy(
            block, sums_hbm.at[kind, step, far], out_sem.at[kind, step, far]
        )
        copy.start()
        out_copies.append(copy)

    def core_sums(step):
        pairs = [(kind, far) for kind in range(3) for far in (1, 0)]
        if step == 1:
            pairs.sort(key=lambda pair: -pair[1])
        for kind, far in pairs:
            over_c(kind, step, far).wait_recv()
            x_at = 1 - me_x if far else me_x
            block = w3.at[kind, row_block(ahead(step), x_at, me_c)]
            add_rows(block, [c_in.at[kind, step, far]], block, rows)
            if step != 1:
                keep(kind, step, far, block)
            elif far:
                over_x(kind).start()

    def first_sums():
        for kind in range(3):
            over_x(kind).wait_recv()
            block = w3.at[kind, row_block(ahead(1), me_x, me_c)]
            add_rows(block, [x_in.at[kind]], block, rows)
            keep(kind, 1, 0, block)

    own_load.wait()
    w_loads(lambda copy: copy.wait())

    @pl.when(outer)
    def _():
        w3[:, :, main:] = jnp.zeros((3, width, units - main), jnp.bfloat16)

    chunk(0)
    forward(1)
    forward(2)
    ag_y_in(1).wait_recv()
    chunk(1)
    ag_y_in(2).wait_recv()
    ag_last().start()
    chunk(2)
    rs_step(1)
    ag_z_in(3).wait_recv()
    ag_last().wait_recv()
    chunk(3)
    rs_y(0).start()
    rs_step(2)
    grads(1)
    grads(2)
    core_sums(1)
    rs_step(3)
    grads(3)
    core_sums(2)
    grads(0)
    core_sums(3)
    rs_step(0)
    core_sums(0)

    cot_load = pltpu.make_async_copy(
        dy_hbm.at[0, mine], dy.at[pl.ds(0, own)], load_sem.at[z_size + 3]
    )
    cot_load.start()
    cot_load.wait()
    mid_load.wait()

    def mid_rows(index, total):
        at = pl.ds(pl.multiple_of(index * 32, 32), 32)
        grad, gain_sum = norm_back(mid[at, :], gain_ref[1:2, :], gm_ref[at, :])
        grad = grad + dy[at, :].astype(jnp.float32)
        gm_ref[at, :] = grad
        dy[pl.ds(pl.multiple_of(own + index * 32, 32), 32), :] = grad.astype(jnp.bfloat16)
        return total + gain_sum

    gain_sum = lax.fori_loop(0, own // 32, mid_rows, jnp.zeros((1, width), jnp.float32))
    gm_save = pltpu.make_async_copy(dy.at[pl.ds(own, own)], gm_hbm, load_sem.at[z_size + 3])
    gm_save.start()
    for index in range(4):
        gain_part[index : index + 1, :] = jnp.zeros((1, span), jnp.float32)
        gain_part[4 + index : 5 + index, :] = gain_sum[:, index * span : (index + 1) * span]
    first_sums()
    gm_save.wait()

    for copy in mix_copies[3:] + out_copies:
        copy.wait()
    for index in range(z_size):
        if index in (1, 2):
            ag_y(index).wait_send()
        if index == 3:
            ag_last().wait_send()
        rs_y(index).wait_send()
        if index < z_size - 1:
            ag_z(index).wait_send()
        if index:
            rs_z(index).wait_send()
        for kind in range(3):
            over_c(kind, index, 0).wait_send()
            over_c(kind, index, 1).wait_send()
            if index == 1:
                over_x(kind).wait_send()


def ffn_call(gains, normed, grad_all, weights, mid, rows, main):
    z_size = lax.axis_size("z")
    pair, width = normed.shape
    units = weights.shape[2]
    own = pair // 2
    wide = lambda *lead: pltpu.VMEM((*lead, width), jnp.bfloat16)
    tall = lambda *lead: pltpu.VMEM((*lead, width, own), jnp.bfloat16)
    dma = lambda *lead: pltpu.SemaphoreType.DMA(lead)
    vmem = pl.BlockSpec(memory_space=pltpu.VMEM)
    hbm = pl.BlockSpec(memory_space=pl.ANY)
    return pl.pallas_call(
        functools.partial(ffn_kernel, z_size, main),
        out_shape=(
            jax.ShapeDtypeStruct((own, width), jnp.float32),
            jax.ShapeDtypeStruct((8, width // z_size), jnp.float32),
            jax.ShapeDtypeStruct((z_size, 2, width, own), jnp.bfloat16),
            jax.ShapeDtypeStruct((3, z_size, 2, rows, units), jnp.bfloat16),
            jax.ShapeDtypeStruct((own, width), jnp.bfloat16),
        ),
        in_specs=[vmem, hbm, hbm, hbm, hbm],
        out_specs=(vmem, vmem, hbm, hbm, hbm),
        scratch_shapes=[
            wide(z_size, pair),
            wide(pair),
            pltpu.VMEM(weights.shape, jnp.bfloat16),
            pltpu.VMEM((3, z_size * pair, units), jnp.bfloat16),
            pltpu.VMEM((width, z_size * pair), jnp.bfloat16),
            pltpu.VMEM((width, z_size * pair), jnp.bfloat16),
            tall(z_size, 2),
            tall(2),
            tall(z_size),
            tall(z_size - 1),
            tall(z_size - 1),
            pltpu.VMEM((3, z_size, 2, rows, units), jnp.bfloat16),
            pltpu.VMEM((3, rows, units), jnp.bfloat16),
            pltpu.VMEM((own, width), jnp.float32),
            dma(z_size + 5),
            dma(z_size),
            dma(z_size, 2),
            dma(z_size, 2),
            dma(z_size, 2),
            dma(z_size, 2),
            dma(z_size, 2),
            dma(z_size, 2),
            dma(z_size, 2),
            dma(z_size, 2),
            dma(3, z_size, 2),
            dma(3, z_size, 2),
            dma(3),
            dma(3),
            dma(3, z_size, 2),
        ],
        compiler_params=pltpu.CompilerParams(
            collective_id=0, has_side_effects=True, vmem_limit_bytes=VMEM_BYTES
        ),
        cost_estimate=pl.CostEstimate(
            flops=18 * z_size * pair * width * units,
            bytes_accessed=4 * weights.size + 12 * z_size * pair * width,
            transcendentals=z_size * pair * units,
        ),
    )(gains, normed, grad_all, weights, mid)


def spin(values, table):
    first = values[:, : values.shape[1] // 2]
    turned = first * table[0] + pltpu.roll(first, first.shape[1] // 2, 1) * table[1]
    return jnp.concatenate([turned, values[:, values.shape[1] // 2 :]], axis=1)


def spin_back(values, table):
    first = values[:, : values.shape[1] // 2]
    turned = first * table[0] - pltpu.roll(first, first.shape[1] // 2, 1) * table[1]
    return jnp.concatenate([turned, values[:, values.shape[1] // 2 :]], axis=1)


def head_probs(rotated, keys, allowed):
    scores = jnp.where(allowed > 0.5, matmul_nt(rotated, keys), masked_score)
    weights = jnp.exp(scores - jnp.max(scores, axis=-1, keepdims=True))
    return weights / jnp.sum(weights, axis=-1, keepdims=True)


def ragged_split(columns, parts):
    main = columns // parts // 128 * 128
    return main, main + 128


def pre_kernel(
    z_size,
    tok_ref,
    wkv_ref,
    gain_one_ref,
    gain_two_ref,
    cos_ref,
    sin_ref,
    seg_ref,
    cot_hbm,
    wq_hbm,
    wo_hbm,
    wg_hbm,
    wu_hbm,
    wd_hbm,
    n1_ref,
    rot_ref,
    key_ref,
    val_ref,
    att_ref,
    mid_ref,
    n2_ref,
    gain_ref,
    allow_ref,
    kv_out,
    wq_out,
    wo_out,
    w3_out,
    dy_out,
    kv_w,
    q_w,
    o_w,
    tok,
    part,
    part_y,
    query,
    gain_rows,
    y_send,
    y_recv,
    ky_send,
    ky_recv,
    az_send,
    az_recv,
    ax_send,
    ax_recv,
    ac_send,
    ac_recv,
    fz_send,
    fz_recv,
    fx_send,
    fx_recv,
    fc_send,
    fc_recv,
    dz_send,
    dz_recv,
    dy_send,
    dy_recv,
    local_sem,
):
    me_z, me_x = lax.axis_index("z"), lax.axis_index("x")
    me_c, me_y = lax.axis_index("c"), lax.axis_index("mp")
    own, width = tok_ref.shape
    rows = wq_hbm.shape[0]
    half_rows = wkv_ref.shape[0]
    head = key_ref.shape[1]
    main, units = ragged_split(wg_hbm.shape[1], z_size)
    to_y, to_x, to_c = {"mp": 1 - me_y}, {"x": 1 - me_x}, {"c": 1 - me_c}

    def to_z(step):
        return {"z": lax.rem(me_z + step, z_size)}

    def from_z(step):
        return lax.rem(me_z - step + z_size, z_size)

    def row_block(step, x_at, c_at):
        start = ((from_z(step) * 2 + x_at) * 2 + c_at) * rows
        return pl.ds(pl.multiple_of(start, rows), rows)

    mine = pl.ds(pl.multiple_of(me_y * own, own), own)
    theirs = pl.ds(pl.multiple_of((1 - me_y) * own, own), own)
    bufs = (kv_w, q_w, o_w)
    inputs = (None, wq_hbm, wo_hbm)

    locals_ = []

    def local(src, dst):
        copy = pltpu.make_async_copy(src, dst, local_sem.at[len(locals_)])
        copy.start()
        locals_.append(copy)
        return copy

    here = row_block(0, me_x, me_c)
    own_q = local(wq_hbm, q_w.at[here])
    own_o = local(wo_hbm, o_w.at[here])
    ffn_in = (wg_hbm, wu_hbm, wd_hbm)

    def body_of(target):
        return pl.ds(pl.multiple_of(target * main, 128), main), pl.ds(0, main)

    def tail_of(target):
        start = z_size * main + lax.rem(target + 1, 2) * 128
        return pl.ds(pl.multiple_of(start, 128), 128), pl.ds(main, 128)

    def is_inner(at):
        return (at > 0) & (at < z_size - 1)

    own_f = []
    for kind in range(3):
        src, dst = body_of(me_z)
        own_f.append(local(ffn_in[kind].at[:, src], w3_out.at[kind, here, dst]))

    def own_tail(kind):
        src, dst = tail_of(me_z)
        return pltpu.make_async_copy(
            ffn_in[kind].at[:, src], w3_out.at[kind, here, dst], local_sem.at[12 + kind]
        )

    @pl.when(is_inner(me_z))
    def _():
        for kind in range(3):
            own_tail(kind).start()
    own_d = local(cot_hbm, dy_out.at[0, mine])

    kv_own = pl.ds(pl.multiple_of(here.start + me_y * half_rows, half_rows), half_rows)
    gain_rows[...] = jnp.zeros(gain_rows.shape, jnp.float32)
    gain_rows[0:1, :half_rows] = gain_one_ref[...].astype(jnp.float32)
    gain_rows[1:2, :half_rows] = gain_two_ref[...].astype(jnp.float32)
    spread = gain_rows[...].T
    kv_w[kv_own, : 2 * head] = wkv_ref[...]
    kv_w[kv_own, 2 * head :] = spread[:half_rows, :].astype(jnp.bfloat16)

    barrier = pltpu.get_barrier_semaphore()
    peers = [to_y, to_x, to_c] + [to_z(step) for step in range(1, z_size)]
    for where in peers:
        pl.semaphore_signal(barrier, inc=1, device_id=where, device_id_type=MESH_ID)
    pl.semaphore_wait(barrier, len(peers))

    tok_y = remote(tok_ref, tok.at[mine], y_send.at[1], y_recv.at[1], to_y)
    tok_y_in = remote(tok_ref, tok.at[theirs], y_send.at[1], y_recv.at[1], to_y)
    part_out = remote(part.at[theirs], part_y, y_send.at[2], y_recv.at[2], to_y)
    n2_y = remote(n2_ref.at[mine], n2_ref.at[mine], y_send.at[3], y_recv.at[3], to_y)
    n2_y_in = remote(n2_ref.at[theirs], n2_ref.at[theirs], y_send.at[3], y_recv.at[3], to_y)

    def block_of(kind, step, x_at):
        if kind:
            return row_block(step, x_at, me_c)
        return kv_rows(step, x_at, me_y)

    def kv_rows(step, x_at, y_at):
        start = row_block(step, x_at, me_c).start + y_at * half_rows
        return pl.ds(pl.multiple_of(start, half_rows), half_rows)

    def kv_y(step, far):
        x_at = 1 - me_x if far else me_x
        block = kv_w.at[kv_rows(step, x_at, me_y)]
        slot = step + z_size * far
        return remote(block, block, ky_send.at[slot], ky_recv.at[slot], to_y)

    def kv_y_in(step, far):
        x_at = 1 - me_x if far else me_x
        block = kv_w.at[kv_rows(step, x_at, 1 - me_y)]
        slot = step + z_size * far
        return remote(block, block, ky_send.at[slot], ky_recv.at[slot], to_y)

    def source(kind, step):
        if isinstance(step, int) and step == 0 and kind:
            return inputs[kind]
        return bufs[kind].at[block_of(kind, step, me_x)]

    first_z, last_z = (z_size - 1 - me_z) // (z_size - 1), me_z // (z_size - 1)
    inner = first_z + last_z == 0
    order = (0, 1 + 2 * first_z, 3 - first_z - last_z, 2 - first_z + last_z)
    hops = (
        None,
        (lax.rem(me_z + 1, z_size), 2),
        (lax.rem(me_z + z_size - 1, z_size), 2),
        (lax.rem(3 * (me_z + 3), z_size), lax.rem(2 * me_z + 3, z_size)),
    )

    def a_z_own(kind, right):
        return remote(
            source(kind, 0),
            bufs[kind].at[block_of(kind, 0, me_x)],
            az_send.at[kind, right],
            az_recv.at[kind, 1 if right else z_size - 1],
            to_z(1 if right else z_size - 1),
        )

    def a_z_start(kind):
        @pl.when(last_z == 0)
        def _():
            a_z_own(kind, 1).start()

        @pl.when(first_z == 0)
        def _():
            a_z_own(kind, 0).start()

    def a_z(kind, index):
        target, slot = hops[index]
        block = bufs[kind].at[block_of(kind, order[index], me_x)]
        return remote(
            block, block, az_send.at[kind, 1 + index], az_recv.at[kind, slot], {"z": target}
        )

    def a_z_next(kind, index):
        @pl.when(inner)
        def _():
            a_z(kind, index).start()

    def a_z_done(kind):
        @pl.when(last_z == 0)
        def _():
            a_z_own(kind, 1).wait_send()

        @pl.when(first_z == 0)
        def _():
            a_z_own(kind, 0).wait_send()

        @pl.when(inner)
        def _():
            for index in range(1, z_size):
                a_z(kind, index).wait_send()

    def a_z_in(kind, step):
        block = bufs[kind].at[block_of(kind, step, me_x)]
        return remote(block, block, az_send.at[kind, 0], az_recv.at[kind, step], to_z(1))

    def a_x(kind, step):
        return remote(
            source(kind, step),
            bufs[kind].at[block_of(kind, step, me_x)],
            ax_send.at[kind, step],
            ax_recv.at[kind, step],
            to_x,
        )

    def a_x_in(kind, step):
        block = bufs[kind].at[block_of(kind, step, 1 - me_x)]
        return remote(block, block, ax_send.at[kind, step], ax_recv.at[kind, step], to_x)

    def a_c(kind, step, far):
        x_at = 1 - me_x if far else me_x
        block = bufs[kind].at[row_block(step, x_at, me_c)]
        src = source(kind, step) if kind and not far else block
        slot = step + z_size * far
        return remote(src, block, ac_send.at[kind, slot], ac_recv.at[kind, slot], to_c)

    def a_c_in(kind, step, far):
        x_at = 1 - me_x if far else me_x
        block = bufs[kind].at[row_block(step, x_at, 1 - me_c)]
        slot = step + z_size * far
        return remote(block, block, ac_send.at[kind, slot], ac_recv.at[kind, slot], to_c)

    def f_z(kind, step, act):
        target = lax.rem(me_z + step, z_size)

        def piece(index, src, dst):
            return remote(
                ffn_in[kind].at[:, src],
                w3_out.at[kind, here, dst],
                fz_send.at[kind, step, index],
                fz_recv.at[kind, step, index],
                to_z(step),
            )

        act(piece(0, *body_of(target)))

        @pl.when(is_inner(target))
        def _():
            act(piece(1, *tail_of(target)))

    def f_z_wait(kind, step):
        block = row_block(step, me_x, me_c)

        def piece(index, dst):
            part = w3_out.at[kind, block, dst]
            return remote(
                part, part, fz_send.at[kind, step, index], fz_recv.at[kind, step, index], to_z(step)
            )

        piece(0, pl.ds(0, main)).wait_recv()

        @pl.when(inner)
        def _():
            piece(1, pl.ds(main, 128)).wait_recv()

    def f_x(kind, step, x_at, act):
        for case, columns in ((inner, units), (first_z + last_z > 0, main)):

            @pl.when(case)
            def _(columns=columns):
                block = w3_out.at[kind, row_block(step, x_at, me_c), pl.ds(0, columns)]
                act(remote(block, block, fx_send.at[kind, step], fx_recv.at[kind, step], to_x))

    def f_x_start(kind, step):
        f_x(kind, step, me_x, lambda copy: copy.start())

    def f_x_wait(kind, step):
        f_x(kind, step, 1 - me_x, lambda copy: copy.wait_recv())

    def f_x_done(kind, step):
        f_x(kind, step, me_x, lambda copy: copy.wait_send())

    def f_c(kind, step, far):
        block = w3_out.at[kind, row_block(step, 1 - me_x if far else me_x, me_c)]
        slot = step + z_size * far
        return remote(block, block, fc_send.at[kind, slot], fc_recv.at[kind, slot], to_c)

    def f_c_in(kind, step, far):
        block = w3_out.at[kind, row_block(step, 1 - me_x if far else me_x, 1 - me_c)]
        slot = step + z_size * far
        return remote(block, block, fc_send.at[kind, slot], fc_recv.at[kind, slot], to_c)

    def d_source(step):
        return cot_hbm if isinstance(step, int) else dy_out.at[step, mine]

    def d_z_own(right):
        slot = 1 if right else z_size - 1
        return remote(
            cot_hbm, dy_out.at[slot, mine], dz_send.at[right], dz_recv.at[slot], to_z(slot)
        )

    def d_z_start():
        @pl.when(last_z == 0)
        def _():
            d_z_own(1).start()

        @pl.when(first_z == 0)
        def _():
            d_z_own(0).start()

    def d_z(index):
        target, slot = hops[index]
        return remote(
            dy_out.at[order[index], mine],
            dy_out.at[slot, mine],
            dz_send.at[1 + index],
            dz_recv.at[slot],
            {"z": target},
        )

    def d_z_done():
        @pl.when(last_z == 0)
        def _():
            d_z_own(1).wait_send()

        @pl.when(first_z == 0)
        def _():
            d_z_own(0).wait_send()

        @pl.when(inner)
        def _():
            for index in range(1, z_size):
                d_z(index).wait_send()

    def d_z_in(step):
        block = dy_out.at[step, mine]
        return remote(block, block, dz_send.at[0], dz_recv.at[step], to_z(1))

    def d_y(step):
        return remote(
            d_source(step), dy_out.at[step, mine], dy_send.at[step], dy_recv.at[step], to_y
        )

    def d_y_in(step):
        block = dy_out.at[step, theirs]
        return remote(block, block, dy_send.at[step], dy_recv.at[step], to_y)

    for kind in (1, 0, 2):
        a_z_start(kind)
        a_x(kind, 0).start()
    kv_y(0, 0).start()
    tok_y.start()
    for kind in (1, 2):
        a_c(kind, 0, 0).start()

    for at_end, away in ((first_z, 1), (last_z, z_size - 1)):

        @pl.when(at_end > 0)
        def _(away=away):
            for kind in range(3):
                f_z(kind, away, lambda copy: copy.start())

    tok[mine, :] = tok_ref[...]
    seq = 2 * own
    query_at = lax.broadcasted_iota(jnp.int32, (seq, seq), 0)
    key_at = lax.broadcasted_iota(jnp.int32, (seq, seq), 1)
    segment = seg_ref[...].astype(jnp.float32)
    same = jnp.broadcast_to(segment, (8, seq)).T[:, :1] == segment
    allowed = same & (key_at <= query_at) & (query_at - key_at < WINDOW)
    allow_ref[...] = jnp.where(allowed, 1.0, 0.0)
    d_y(0).start()

    def from_x(index):
        step = order[index]
        for kind in (1, 0, 2):
            a_x_in(kind, step).wait_recv()
            if kind:
                a_c(kind, step, 1).start()
            else:
                kv_y(step, 1).start()

    def from_y(index):
        step = order[index]
        for far in range(2):
            kv_y_in(step, far).wait_recv()
            a_c(0, step, far).start()

    for index in range(1, z_size):
        step = order[index]
        for kind in (1, 0, 2):
            a_z_in(kind, step).wait_recv()
            a_z_next(kind, index)
            a_x(kind, step).start()
            if kind:
                a_c(kind, step, 0).start()
            else:
                kv_y(step, 0).start()
        if index == z_size - 2:
            d_z_start()
        if index == z_size - 1:
            for copy in own_f:
                copy.wait()

            @pl.when(inner)
            def _():
                for kind in range(3):
                    own_tail(kind).wait()

            for kind in range(3):
                for away, sent in ((1, first_z), (3, last_z), (2, 0)):

                    @pl.when(sent == 0 if away != 2 else me_z >= 0)
                    def _(kind=kind, away=away):
                        f_z(kind, away, lambda copy: copy.start())

            for kind in range(3):
                f_x_start(kind, 0)
                f_c(kind, 0, 0).start()
        if index >= 2:
            from_x(index - 2)
            from_y(index - 2)
    for index in (z_size - 2, z_size - 1):
        from_x(index)
        from_y(index)

    def hand_on(kind, step):
        f_z_wait(kind, step)
        f_x_start(kind, step)
        f_c(kind, step, 0).start()

    def cross(kind, step):
        f_x_wait(kind, step)
        f_c(kind, step, 1).start()

    def pass_cotangent(step):
        d_z_in(order[step]).wait_recv()

        @pl.when(inner)
        def _():
            d_z(step).start()

        d_y(order[step]).start()

    def pass_if(case, step):
        @pl.when(case)
        def _():
            pass_cotangent(step)

    outer = first_z + last_z > 0
    tok_y_in.wait_recv()
    own_q.wait()
    own_o.wait()
    for kind in (0, 1):
        for step in range(z_size):
            for far in range(2):
                a_c_in(kind, step, far).wait_recv()

    gains = kv_w[:, 2 * head :].astype(jnp.float32).T[:8, :]
    gain_ref[...] = gains

    def norm_rows(index, carry):
        at = pl.ds(pl.multiple_of(index * 32, 32), 32)
        values = tok[at, :].astype(jnp.float32)
        scale = lax.rsqrt(jnp.mean(values * values, axis=-1, keepdims=True) + epsilon)
        n1_ref[at, :] = (values * scale * gain_ref[0:1, :]).astype(jnp.bfloat16)
        return carry

    lax.fori_loop(0, 2 * own // 32, norm_rows, 0)
    hand_on(0, order[1])
    table = (cos_ref[...], sin_ref[...])
    key_ref[...] = spin(dot_nn(n1_ref[...], kv_w[:, :head]), table).astype(jnp.bfloat16)
    val_ref[...] = dot_nn(n1_ref[...], kv_w[:, head : 2 * head]).astype(jnp.bfloat16)
    hand_on(0, order[2])
    head_scale = head ** (-0.5)
    heads = att_ref.shape[1] // head

    half_cols = att_ref.shape[1] // 2
    for index in range(2):
        cols = pl.ds(index * half_cols, half_cols)
        query[:, cols] = dot_nn(n1_ref[...], q_w[:, cols])

    def attend(index):
        cols = pl.ds(index * head, head)
        rotated = (spin(query[:, cols], table) * head_scale).astype(jnp.bfloat16)
        rot_ref[:, cols] = rotated
        probs = head_probs(rotated, key_ref[...], allow_ref[...]).astype(jnp.bfloat16)
        att_ref[:, cols] = dot_nn(probs, val_ref[...]).astype(jnp.bfloat16)

    tasks = [
        lambda: (pass_cotangent(1), pass_if(inner, 2)),
        lambda: hand_on(0, order[3]),
        lambda: (cross(0, 0), hand_on(1, order[1])),
        lambda: cross(1, 0),
        lambda: (cross(2, 0), hand_on(1, order[2])),
    ]
    for index in range(heads):
        attend(index)
        if index < len(tasks):
            tasks[index]()
    for step in range(z_size):
        for far in range(2):
            a_c_in(2, step, far).wait_recv()
    saves = [
        local(kv_w, kv_out),
        local(q_w, wq_out),
        local(o_w, wo_out),
    ]
    span = width // 4

    def project(index, carry):
        cols = pl.ds(pl.multiple_of(index * span, span), span)
        part[:, cols] = matmul_nt(att_ref[...], o_w[cols, :]).astype(jnp.bfloat16)
        return carry

    lax.fori_loop(0, 4, project, 0)
    part_out.start()
    hand_on(1, order[3])
    pass_if(outer, 2)
    pass_if(inner, 3)
    cross(0, order[1])
    hand_on(2, order[1])
    part_out.wait_recv()

    def middle(index, carry):
        at = pl.ds(pl.multiple_of(index * 32, 32), 32)
        there = pl.ds(pl.multiple_of(me_y * own + index * 32, 32), 32)
        values = (
            tok_ref[at, :].astype(jnp.float32)
            + part[there, :].astype(jnp.float32)
            + part_y[at, :].astype(jnp.float32)
        )
        mid_ref[at, :] = values
        scale = lax.rsqrt(jnp.mean(values * values, axis=-1, keepdims=True) + epsilon)
        n2_ref[there, :] = (values * scale * gain_ref[1:2, :]).astype(jnp.bfloat16)
        return carry

    lax.fori_loop(0, own // 32, middle, 0)
    n2_y.start()
    hand_on(2, order[2])
    cross(0, order[2])
    cross(0, order[3])
    hand_on(2, order[3])
    pass_if(outer, 3)
    for kind in (1, 2):
        for index in (1, 2, 3):
            cross(kind, order[index])
    for kind in range(3):
        for step in range(z_size):
            for far in range(2):
                f_c_in(kind, step, far).wait_recv()
    for step in range(z_size):
        d_y_in(step).wait_recv()
    n2_y_in.wait_recv()

    for kind in range(3):
        a_z_done(kind)
    d_z_done()
    tok_y.wait_send()
    part_out.wait_send()
    n2_y.wait_send()
    own_d.wait()
    for copy in saves:
        copy.wait()
    for step in range(z_size):
        d_y(step).wait_send()
        for far in range(2):
            kv_y(step, far).wait_send()
        for kind in range(3):
            if step:
                f_z(kind, step, lambda copy: copy.wait_send())
            a_x(kind, step).wait_send()
            f_x_done(kind, step)
            for far in range(2):
                a_c(kind, step, far).wait_send()
                f_c(kind, step, far).wait_send()


def pre_call(
    tokens, w_kv, gain_one, gain_two, table, segments, cotangent, w_query, w_out, ffn
):
    z_size = lax.axis_size("z")
    own, width = tokens.shape
    seq = 2 * own
    rows, cols = w_query.shape
    head = table[0].shape[1] * 2
    units = ragged_split(ffn[0].shape[1], z_size)[1]
    low = lambda *dims: jax.ShapeDtypeStruct(dims, jnp.bfloat16)
    full = lambda *dims: jax.ShapeDtypeStruct(dims, jnp.float32)
    dma = lambda *lead: pltpu.SemaphoreType.DMA(lead)
    vmem = pl.BlockSpec(memory_space=pltpu.VMEM)
    hbm = pl.BlockSpec(memory_space=pl.ANY)
    wide = lambda *lead: pltpu.VMEM((*lead, width), jnp.bfloat16)
    return pl.pallas_call(
        functools.partial(pre_kernel, z_size),
        out_shape=(
            low(seq, width),
            low(seq, cols),
            low(seq, head),
            low(seq, head),
            low(seq, cols),
            full(own, width),
            low(seq, width),
            full(8, width),
            full(seq, seq),
            low(width, 2 * head + 128),
            low(width, cols),
            low(width, cols),
            low(3, width, units),
            low(z_size, seq, width),
        ),
        in_specs=[vmem] * 7 + [hbm] * 6,
        out_specs=(vmem,) * 9 + (hbm,) * 5,
        scratch_shapes=[
            pltpu.VMEM((width, 2 * head + 128), jnp.bfloat16),
            pltpu.VMEM((width, cols), jnp.bfloat16),
            pltpu.VMEM((width, cols), jnp.bfloat16),
            wide(seq),
            wide(seq),
            wide(own),
            pltpu.VMEM((seq, cols), jnp.float32),
            pltpu.VMEM((128, 128), jnp.float32),
            dma(4),
            dma(4),
            dma(2 * z_size),
            dma(2 * z_size),
            dma(3, z_size + 1),
            dma(3, z_size),
            dma(3, z_size),
            dma(3, z_size),
            dma(3, 2 * z_size),
            dma(3, 2 * z_size),
            dma(3, z_size, 2),
            dma(3, z_size, 2),
            dma(3, z_size),
            dma(3, z_size),
            dma(3, 2 * z_size),
            dma(3, 2 * z_size),
            dma(z_size + 1),
            dma(z_size),
            dma(z_size),
            dma(z_size),
            dma(16),
        ],
        compiler_params=pltpu.CompilerParams(
            collective_id=1, has_side_effects=True, vmem_limit_bytes=VMEM_BYTES
        ),
        cost_estimate=pl.CostEstimate(
            flops=8 * seq * width * cols,
            bytes_accessed=8 * width * (cols + units),
            transcendentals=seq * seq * cols // head,
        ),
    )(tokens, w_kv, gain_one, gain_two, *table, segments, cotangent, w_query, w_out, *ffn)


def post_kernel(
    z_size,
    main,
    tok_ref,
    gain_ref,
    gain_part_ref,
    n1_ref,
    rot_ref,
    key_ref,
    val_ref,
    att_ref,
    cos_ref,
    sin_ref,
    allow_ref,
    kv_hbm,
    wq_hbm,
    wo_hbm,
    mix_hbm,
    gmf_hbm,
    gmb_hbm,
    mid_hbm,
    sums_hbm,
    mixed_ref,
    tgrad_ref,
    gsum_ref,
    kvg_ref,
    qg_ref,
    og_ref,
    ffn_out,
    kv_w,
    q_w,
    o_w,
    o_part,
    gm,
    gm_f,
    gq,
    gkv,
    kv_sum,
    back_y,
    mix_y,
    mix_z,
    mix_s,
    o_c,
    o_x,
    o_z,
    q_c,
    q_x,
    q_z,
    kv_y,
    kv_c,
    kv_x,
    kv_z,
    gain_own,
    gain_in,
    ffn_in,
    ffn_own,
    load_sem,
    own_sem,
    fx_send,
    fx_recv,
    fz_send,
    fz_recv,
    y_send,
    y_recv,
    my_send,
    my_recv,
    mz_send,
    mz_recv,
    wc_send,
    wc_recv,
    wx_send,
    wx_recv,
    wz_send,
    wz_recv,
    kc_send,
    kc_recv,
    kz_send,
    kz_recv,
    g_send,
    g_recv,
):
    me_z, me_x = lax.axis_index("z"), lax.axis_index("x")
    me_c, me_y = lax.axis_index("c"), lax.axis_index("mp")
    own, width = tok_ref.shape
    seq = 2 * own
    head = key_ref.shape[1]
    cols_here = att_ref.shape[1]
    heads = cols_here // head
    rows = qg_ref.shape[0]
    span = width // z_size
    mine = pl.ds(pl.multiple_of(me_y * own, own), own)
    theirs = pl.ds(pl.multiple_of((1 - me_y) * own, own), own)
    to_y, to_x, to_c = {"mp": 1 - me_y}, {"x": 1 - me_x}, {"c": 1 - me_c}
    head_scale = head ** (-0.5)

    def behind(step):
        return lax.rem(me_z - step + z_size, z_size)

    def to_z(step):
        return {"z": lax.rem(me_z + step, z_size)}

    def row_block(step, x_at, c_at):
        start = ((behind(step) * 2 + x_at) * 2 + c_at) * rows
        return pl.ds(pl.multiple_of(start, rows), rows)

    loads = [
        pltpu.make_async_copy(wo_hbm, o_w, load_sem.at[0]),
        pltpu.make_async_copy(wq_hbm, q_w, load_sem.at[1]),
        pltpu.make_async_copy(
            kv_hbm.at[:, :, :, :, :, pl.ds(0, 2 * head)], kv_w, load_sem.at[2]
        ),
    ]
    for step in range(z_size):
        loads.append(
            pltpu.make_async_copy(mix_hbm.at[step, me_y], mix_s.at[step], load_sem.at[3 + step])
        )
    loads.append(pltpu.make_async_copy(gmf_hbm, gm_f, load_sem.at[3 + z_size]))
    loads.append(pltpu.make_async_copy(gmb_hbm, gm.at[mine], load_sem.at[4 + z_size]))
    mid_load = pltpu.make_async_copy(mid_hbm, gm_f, load_sem.at[5 + z_size])
    for load in loads:
        load.start()

    barrier = pltpu.get_barrier_semaphore()
    peers = [to_y, to_x, to_c] + [to_z(step) for step in range(1, z_size)]
    for where in peers:
        pl.semaphore_signal(barrier, inc=1, device_id=where, device_id_type=MESH_ID)
    pl.semaphore_wait(barrier, len(peers))

    tasks = [(step, kind) for step in (2, 3) for kind in range(3)]

    def f_x(index):
        step, kind = tasks[index]
        return remote(
            sums_hbm.at[kind, step, 1],
            ffn_in.at[index],
            fx_send.at[index],
            fx_recv.at[index],
            to_x,
        )

    def f_own(index):
        step, kind = tasks[index]
        return pltpu.make_async_copy(
            sums_hbm.at[kind, step, 0], ffn_own.at[index % 2], own_sem.at[index % 2]
        )

    def f_z(step, kind, source_z, act):
        for case, columns in (
            ((source_z > 0) & (source_z < z_size - 1), ffn_out.shape[3]),
            ((source_z == 0) | (source_z == z_size - 1), main),
        ):

            @pl.when(case)
            def _(columns=columns):
                cols = pl.ds(0, columns)
                if step == 1:
                    src = sums_hbm.at[kind, 1, 0, :, cols]
                else:
                    src = ffn_in.at[tasks.index((step, kind)), :, cols]
                act(
                    remote(
                        src,
                        ffn_out.at[kind, step, :, cols],
                        fz_send.at[kind, step],
                        fz_recv.at[kind, step],
                        to_z(step),
                    )
                )

    def tick(index):
        step, kind = tasks[index]
        f_x(index).wait_recv()
        f_own(index).wait()
        block = ffn_in.at[index]
        add_rows(block, [ffn_own.at[index % 2]], block, rows)
        if index + 2 < len(tasks):
            f_own(index + 2).start()
        f_z(step, kind, me_z, lambda copy: copy.start())

    def f_x_own(kind):
        return remote(
            sums_hbm.at[kind, 0, 1],
            ffn_out.at[kind, 0],
            fx_send.at[len(tasks) + kind],
            fx_recv.at[len(tasks) + kind],
            to_x,
        )

    f_own(0).start()
    f_own(1).start()
    for index in range(len(tasks)):
        f_x(index).start()
    for kind in range(3):
        f_z(1, kind, me_z, lambda copy: copy.start())

    gm_y = remote(gmb_hbm, gm.at[mine], y_send.at[0], y_recv.at[0], to_y)
    gm_y_in = remote(gm.at[theirs], gm.at[theirs], y_send.at[0], y_recv.at[0], to_y)
    gm_y.start()

    first_z, last_z = (z_size - 1 - me_z) // (z_size - 1), me_z // (z_size - 1)
    inner = first_z + last_z == 0
    order = (
        0,
        1 + (me_z + 1) // 2,
        2 + (2 * me_z - 3) * (1 - first_z - last_z),
        3 - 2 * (me_z // 2),
    )
    right = (None, 1 - me_z // 2, (3 - me_z) * (2 - me_z) // 6 + me_z // 2 * (1 - last_z), 1 - me_z // 2)

    def hop_slot(index):
        step, way = order[index], right[index]
        return way * lax.rem(step + 1, z_size) + (1 - way) * (step - 1 + 4 * ((3 - step) // 2))

    def hop_target(index):
        return {"z": me_z + 2 * right[index] - 1}

    def mix_over_y(step):
        return remote(
            mix_hbm.at[step, 1 - me_y], mix_y.at[step], my_send.at[step], my_recv.at[step], to_y
        )

    def mix_over_z(index):
        slot = hop_slot(index)
        return remote(
            mix_s.at[order[index]],
            mix_z.at[slot],
            mz_send.at[index],
            mz_recv.at[slot],
            hop_target(index),
        )

    def mix_z_in(slot):
        return remote(mix_z.at[slot], mix_z.at[slot], mz_send.at[1], mz_recv.at[slot], to_z(1))

    def mix_add(step, others, last):
        def add_tile(tile, carry):
            at = pl.ds(pl.multiple_of(tile * TILE, TILE), TILE)
            total = mix_s[step, at, :].astype(jnp.float32)
            for other in others:
                total = total + other[at, :].astype(jnp.float32)
            if last:
                mixed_ref[:, at] = (gm_f[:, at] + total.T).astype(jnp.bfloat16)
            else:
                mix_s[step, at, :] = total.astype(jnp.bfloat16)
            return carry

        lax.fori_loop(0, width // TILE, add_tile, 0)

    def mix_step(index):
        step = order[index]
        mix_over_y(step).wait_recv()
        from_y = mix_y.at[step]
        if index:

            @pl.when(inner)
            def _():
                mix_z_in(step).wait_recv()
                mix_add(step, [from_y, mix_z.at[step]], False)

            @pl.when(first_z + last_z > 0)
            def _():
                mix_add(step, [from_y], False)

            mix_over_z(index).start()
        else:
            mid_load.wait()

            @pl.when(first_z == 0)
            def _():
                mix_z_in(0).wait_recv()

            @pl.when(last_z == 0)
            def _():
                mix_z_in(z_size).wait_recv()

            @pl.when(inner)
            def _():
                mix_add(0, [from_y, mix_z.at[0], mix_z.at[z_size]], True)

            @pl.when(first_z > 0)
            def _():
                mix_add(0, [from_y, mix_z.at[z_size]], True)

            @pl.when(last_z > 0)
            def _():
                mix_add(0, [from_y, mix_z.at[0]], True)

    for index in (1, 2, 3, 0):
        mix_over_y(order[index]).start()

    kinds = ((o_part, o_c, o_x, o_z, og_ref), (o_w, q_c, q_x, q_z, qg_ref))

    def w_c(kind, step, far):
        x_at = 1 - me_x if far else me_x
        return remote(
            kinds[kind][0].at[row_block(step, x_at, 1 - me_c)],
            kinds[kind][1].at[step, far],
            wc_send.at[kind, step, far],
            wc_recv.at[kind, step, far],
            to_c,
        )

    def w_x(kind, step):
        return remote(
            kinds[kind][0].at[row_block(step, 1 - me_x, me_c)],
            kinds[kind][2].at[step],
            wx_send.at[kind, step],
            wx_recv.at[kind, step],
            to_x,
        )

    def w_z(kind, index):
        step, slot = order[index], hop_slot(index)
        return remote(
            kinds[kind][0].at[row_block(step, me_x, me_c)],
            kinds[kind][3].at[slot],
            wz_send.at[kind, index],
            wz_recv.at[kind, slot],
            hop_target(index),
        )

    def w_z_in(kind, slot):
        block = kinds[kind][3].at[slot]
        return remote(block, block, wz_send.at[kind, 1], wz_recv.at[kind, slot], to_z(1))

    def w_x_stage(kind, index):
        step = order[index]
        w_c(kind, step, 1).wait_recv()
        block = kinds[kind][0].at[row_block(step, 1 - me_x, me_c)]
        add_rows(block, [kinds[kind][1].at[step, 1]], block, rows)
        w_x(kind, step).start()

    def w_z_stage(kind, index):
        part, from_c, from_x, from_z, result = kinds[kind]
        step = order[index]
        w_c(kind, step, 0).wait_recv()
        w_x(kind, step).wait_recv()
        block = part.at[row_block(step, me_x, me_c)]
        others = [from_c.at[step, 0], from_x.at[step]]
        if index:

            @pl.when(inner)
            def _():
                w_z_in(kind, step).wait_recv()
                add_rows(block, [*others, from_z.at[step]], block, rows)

            @pl.when(first_z + last_z > 0)
            def _():
                add_rows(block, others, block, rows)

            w_z(kind, index).start()
        else:

            @pl.when(first_z == 0)
            def _():
                w_z_in(kind, 0).wait_recv()

            @pl.when(last_z == 0)
            def _():
                w_z_in(kind, z_size).wait_recv()

            @pl.when(inner)
            def _():
                add_rows(block, [*others, from_z.at[0], from_z.at[z_size]], result, rows)

            @pl.when(first_z > 0)
            def _():
                add_rows(block, [*others, from_z.at[z_size]], result, rows)

            @pl.when(last_z > 0)
            def _():
                add_rows(block, [*others, from_z.at[0]], result, rows)

    def w_product(kind, index, left, values):
        step = order[index]
        at = pl.ds(pl.multiple_of(behind(step) * span, 128), span)
        turned = left[:, at].T

        def tile_body(tile, carry):
            cols = pl.ds(pl.multiple_of(tile * TILE, TILE), TILE)
            kinds[kind][0][at, cols] = dot_nn(turned, values[:, cols]).astype(jnp.bfloat16)
            return carry

        lax.fori_loop(0, cols_here // TILE, tile_body, 0)
        for far in (1, 0):
            w_c(kind, step, far).start()

    tick(0)
    tick(1)
    loads[-1].wait()
    gm_y_in.wait_recv()
    w_product(0, 1, gm, att_ref)
    w_product(0, 2, gm, att_ref)
    w_x_stage(0, 1)
    w_product(0, 3, gm, att_ref)
    w_x_stage(0, 2)
    tick(2)
    w_product(0, 0, gm, att_ref)
    w_x_stage(0, 3)
    for load in loads[:-1]:
        load.wait()

    kv_sum[...] = jnp.zeros(kv_sum.shape, jnp.float32)
    table = (cos_ref[...], sin_ref[...])

    for index in range(2):
        cols = pl.ds(index * (cols_here // 2), cols_here // 2)
        gq[:, cols] = dot_nn(gm[...], o_w[:, cols]).astype(jnp.bfloat16)

    def attend_back(index):
        cols = pl.ds(index * head, head)
        grad_vals = gq[:, cols]
        rotated = rot_ref[:, cols]
        probs = head_probs(rotated, key_ref[...], allow_ref[...])
        grad_probs = matmul_nt(grad_vals, val_ref[...])
        delta = jnp.sum(probs * grad_probs, axis=-1, keepdims=True)
        grad_scores = (probs * (grad_probs - delta)).astype(jnp.bfloat16)
        grad_rot = dot_nn(grad_scores, key_ref[...])
        gq[:, cols] = (spin_back(grad_rot, table) * head_scale).astype(jnp.bfloat16)
        kv_sum[0] += matmul_tn(grad_scores, rotated)
        kv_sum[1] += matmul_tn(probs.astype(jnp.bfloat16), grad_vals)

    for index in range(heads):
        attend_back(index)
        if index == 0:
            w_x_stage(0, 0)
        if 3 + index < len(tasks):
            tick(3 + index)
        if index == heads - 1:
            mix_step(1)
    gkv[:, :head] = spin_back(kv_sum[0], table).astype(jnp.bfloat16)
    gkv[:, head:] = kv_sum[1].astype(jnp.bfloat16)

    w_product(1, 1, n1_ref, gq)
    w_product(1, 2, n1_ref, gq)
    w_x_stage(1, 1)
    w_z_stage(0, 1)
    w_product(1, 3, n1_ref, gq)
    w_x_stage(1, 2)
    w_product(1, 0, n1_ref, gq)
    w_x_stage(1, 3)
    w_x_stage(1, 0)
    for kind in range(3):
        f_x_own(kind).start()

    gm_y.wait_send()
    back = gm
    def input_tile(index, carry):
        at = pl.ds(pl.multiple_of(index * span, 128), span)
        back[:, at] = (
            matmul_nt(gq[...], q_w[at, :]) + matmul_nt(gkv[...], kv_w[index].reshape(span, 2 * head))
        ).astype(jnp.bfloat16)
        return carry

    lax.fori_loop(0, z_size, input_tile, 0)
    back_out = remote(back.at[theirs], back_y, y_send.at[1], y_recv.at[1], to_y)
    back_out.start()

    kv_part = kv_w

    def kv_tile(index, carry):
        at = pl.ds(pl.multiple_of(index * span, 128), span)
        product = dot_nn(n1_ref[:, at].T, gkv[...]).astype(jnp.bfloat16)
        kv_part[index] = product.reshape(kv_part.shape[1:])
        return carry

    lax.fori_loop(0, z_size, kv_tile, 0)
    kv_over_y = remote(kv_part.at[:, :, :, 1 - me_y], kv_y, y_send.at[2], y_recv.at[2], to_y)
    kv_over_y.start()
    mix_step(2)
    w_z_stage(0, 2)
    mix_step(3)
    w_z_stage(0, 3)

    back_out.wait_recv()

    def input_rows(index, total):
        at = pl.ds(pl.multiple_of(index * 32, 32), 32)
        there = pl.ds(pl.multiple_of(me_y * own + index * 32, 32), 32)
        upstream = back[there, :].astype(jnp.float32) + back_y[at, :].astype(jnp.float32)
        grad, gain_part = norm_back(
            tok_ref[at, :].astype(jnp.float32), gain_ref[0:1, :], upstream
        )
        tgrad_ref[at, :] = (gm_f[at, :] + grad).astype(jnp.bfloat16)
        return total + gain_part

    attn_gain_part = lax.fori_loop(
        0, own // 32, input_rows, jnp.zeros((1, width), jnp.float32)
    )
    for index in range(4):
        at = slice(index * span, (index + 1) * span)
        gain_own[0, index : index + 1, :] = attn_gain_part[:, at]
        gain_own[0, 4 + index : 5 + index, :] = gain_part_ref[4 + index : 5 + index, :]

    def gain_send(stage, where):
        return remote(
            gain_own.at[stage], gain_in.at[stage], g_send.at[stage], g_recv.at[stage], where
        )

    gain_hops = [gain_send(0, to_y), gain_send(1, to_c), gain_send(2, to_x)]
    gain_last = [
        remote(
            gain_own.at[3], gain_in.at[2 + step], g_send.at[2 + step], g_recv.at[2 + step], to_z(step)
        )
        for step in range(1, z_size)
    ]

    def gain_fold(stage):
        gain_hops[stage].wait_recv()
        gain_own[stage + 1] = gain_own[stage] + gain_in[stage]

    gain_hops[0].start()
    mid_load.start()
    w_z_stage(1, 1)
    w_z_stage(0, 0)
    w_z_stage(1, 2)
    gain_fold(0)
    gain_hops[1].start()
    mix_step(0)
    w_z_stage(1, 3)
    gain_fold(1)
    gain_hops[2].start()
    kv_over_y.wait_recv()

    def kv_add_y(index, carry):
        for x_at in range(2):
            for c_at in range(2):
                block = kv_part.at[index, x_at, c_at, me_y]
                block[...] = (
                    block[...].astype(jnp.float32) + kv_y[index, x_at, c_at].astype(jnp.float32)
                ).astype(jnp.bfloat16)
        return carry

    lax.fori_loop(0, z_size, kv_add_y, 0)
    kv_over_c = remote(
        kv_part.at[:, :, 1 - me_c, me_y], kv_c, kc_send.at[0], kc_recv.at[0], to_c
    )
    kv_over_c.start()
    gain_fold(2)
    for copy in gain_last:
        copy.start()
    kv_over_c.wait_recv()

    def kv_add_c(index, carry):
        for x_at in range(2):
            block = kv_part.at[index, x_at, me_c, me_y]
            block[...] = (
                block[...].astype(jnp.float32) + kv_c[index, x_at].astype(jnp.float32)
            ).astype(jnp.bfloat16)
        return carry

    lax.fori_loop(0, z_size, kv_add_c, 0)
    kv_over_x = remote(
        kv_part.at[:, 1 - me_x, me_c, me_y], kv_x, kc_send.at[1], kc_recv.at[1], to_x
    )
    kv_over_x.start()
    w_z_stage(1, 0)
    kv_over_x.wait_recv()

    def kv_add_x(index, carry):
        block = kv_part.at[index, me_x, me_c, me_y]
        block[...] = (
            block[...].astype(jnp.float32) + kv_x[index].astype(jnp.float32)
        ).astype(jnp.bfloat16)
        return carry

    lax.fori_loop(0, z_size, kv_add_x, 0)
    kv_over_z = [
        remote(
            kv_part.at[lax.rem(me_z + step, z_size), me_x, me_c, me_y],
            kv_z.at[step - 1],
            kz_send.at[step],
            kz_recv.at[step],
            to_z(step),
        )
        for step in range(1, z_size)
    ]
    for copy in kv_over_z:
        copy.start()
    for copy in gain_last:
        copy.wait_recv()
    gsum_ref[...] = gain_own[3] + gain_in[3] + gain_in[4] + gain_in[5]
    for copy in kv_over_z:
        copy.wait_recv()
    kvg_ref[...] = (
        kv_part[me_z, me_x, me_c, me_y].astype(jnp.float32)
        + kv_z[0].astype(jnp.float32)
        + kv_z[1].astype(jnp.float32)
        + kv_z[2].astype(jnp.float32)
    )

    back_out.wait_send()
    kv_over_y.wait_send()
    kv_over_c.wait_send()
    kv_over_x.wait_send()
    for kind in range(3):
        f_x_own(kind).wait()
    for index in range(len(tasks)):
        f_x(index).wait_send()
    for step in range(1, z_size):
        for kind in range(3):
            f_z(step, kind, me_z, lambda copy: copy.wait_send())
            f_z(step, kind, behind(step), lambda copy: copy.wait_recv())
    for copy in gain_hops + gain_last + kv_over_z:
        copy.wait_send()
    for step in range(z_size):
        mix_over_y(step).wait_send()
        if step:
            mix_over_z(step).wait_send()
        for kind in range(2):
            w_c(kind, step, 0).wait_send()
            w_c(kind, step, 1).wait_send()
            w_x(kind, step).wait_send()
            if step:
                w_z(kind, step).wait_send()


def post_call(
    tokens,
    gains,
    gain_part,
    normed_one,
    rotated,
    keys,
    values,
    attn_vals,
    table,
    allowed,
    kv_weight,
    query_weight,
    out_weight,
    mix_parts,
    grad_mid,
    grad_mid_low,
    mid,
    ffn_sums,
    main,
):
    z_size = lax.axis_size("z")
    own, width = tokens.shape
    seq = 2 * own
    head = keys.shape[1]
    cols = attn_vals.shape[1]
    rows = width // (4 * z_size)
    units = ffn_sums.shape[4]
    low = lambda *dims: pltpu.VMEM(dims, jnp.bfloat16)
    full = lambda *dims: pltpu.VMEM(dims, jnp.float32)
    out_full = lambda *dims: jax.ShapeDtypeStruct(dims, jnp.float32)
    out_low = lambda *dims: jax.ShapeDtypeStruct(dims, jnp.bfloat16)
    dma = lambda *lead: pltpu.SemaphoreType.DMA(lead)
    vmem = pl.BlockSpec(memory_space=pltpu.VMEM)
    hbm = pl.BlockSpec(memory_space=pl.ANY)
    z = z_size
    return pl.pallas_call(
        functools.partial(post_kernel, z_size, main),
        out_shape=(
            out_low(own, width),
            out_low(own, width),
            out_full(8, width // z),
            out_full(rows // 2, 2 * head),
            out_full(rows, cols),
            out_full(rows, cols),
            out_low(3, z, rows, units),
        ),
        in_specs=[vmem] * 11 + [hbm] * 8,
        out_specs=(vmem,) * 6 + (hbm,),
        scratch_shapes=[
            low(z, 2, 2, 2, rows // 2, 2 * head),
            low(width, cols),
            low(width, cols),
            low(width, cols),
            low(seq, width),
            full(own, width),
            low(seq, cols),
            low(seq, 2 * head),
            full(2, seq, head),
            low(own, width),
            low(z, width, own),
            low(z + 1, width, own),
            low(z, width, own),
            low(z, 2, rows, cols),
            low(z, rows, cols),
            low(z + 1, rows, cols),
            low(z, 2, rows, cols),
            low(z, rows, cols),
            low(z + 1, rows, cols),
            low(z, 2, 2, rows // 2, 2 * head),
            low(z, 2, rows // 2, 2 * head),
            low(z, rows // 2, 2 * head),
            low(z - 1, rows // 2, 2 * head),
            full(4, 8, width // z),
            full(6, 8, width // z),
            low(6, rows, units),
            low(2, rows, units),
            dma(6 + z),
            dma(2),
            dma(9),
            dma(9),
            dma(3, z),
            dma(3, z),
            dma(3),
            dma(3),
            dma(z),
            dma(z),
            dma(z),
            dma(z + 1),
            dma(2, z, 2),
            dma(2, z, 2),
            dma(2, z),
            dma(2, z),
            dma(2, z),
            dma(2, z + 1),
            dma(2),
            dma(2),
            dma(z),
            dma(z),
            dma(6),
            dma(6),
        ],
        compiler_params=pltpu.CompilerParams(
            collective_id=2, has_side_effects=True, vmem_limit_bytes=VMEM_BYTES
        ),
        cost_estimate=pl.CostEstimate(
            flops=14 * seq * width * cols,
            bytes_accessed=10 * width * cols,
            transcendentals=seq * seq * cols // head,
        ),
    )(
        tokens,
        gains,
        gain_part,
        normed_one,
        rotated,
        keys,
        values,
        attn_vals,
        *table,
        allowed,
        kv_weight.reshape(z, 2, 2, 2, rows // 2, kv_weight.shape[1]),
        query_weight,
        out_weight,
        mix_parts,
        grad_mid,
        grad_mid_low,
        mid,
        ffn_sums,
    )


def layout_kernel(
    z_size,
    main,
    sum_ref,
    ffn_ref,
    q_ref,
    o_ref,
    kv_ref,
    mixed_in,
    tgrad_in,
    wg_ref,
    wu_ref,
    wd_ref,
    qg_ref,
    og_ref,
    kvg_ref,
    mixed_ref,
    tgrad_ref,
):
    me_z = lax.axis_index("z")
    for kind, out in enumerate((wg_ref, wu_ref, wd_ref)):
        for step in range(z_size):
            at = lax.rem(me_z - step + z_size, z_size)
            values = ffn_ref[kind, step].astype(jnp.float32)
            if step == 0:
                values = values + sum_ref[kind, 0, 0].astype(jnp.float32)
            body = pl.ds(pl.multiple_of(at * main, 128), main)
            out[:, body] = values[:, :main]

            @pl.when((at > 0) & (at < z_size - 1))
            def _(out=out, at=at, values=values):
                tail = z_size * main + lax.rem(at + 1, 2) * 128
                out[:, pl.ds(pl.multiple_of(tail, 128), 128)] = values[:, main:]
    qg_ref[...] = q_ref[...]
    og_ref[...] = o_ref[...]
    kvg_ref[...] = kv_ref[...]
    mixed_ref[...] = mixed_in[...]
    tgrad_ref[...] = tgrad_in[...]


def layout_call(ffn_sums, ffn_grads, query_grad, out_grad, kv_grad, mixed, tokens_grad, ffn_cols):
    z_size = lax.axis_size("z")
    main, units = ragged_split(ffn_cols, z_size)
    rows, cols = query_grad.shape
    parts = rows // 80
    kv_rows = kv_grad.shape[0] // parts
    full = lambda *dims: jax.ShapeDtypeStruct(dims, jnp.float32)
    row = lambda height, width: pl.BlockSpec((height, width), lambda index: (index, 0))
    own, width = mixed.shape
    share = pl.BlockSpec((own, width // parts), lambda index: (0, index))
    specs = [row(80, cols), row(80, cols), row(kv_rows, kv_grad.shape[1]), share, share]
    return pl.pallas_call(
        functools.partial(layout_kernel, z_size, main),
        grid=(parts,),
        out_shape=(
            *[full(rows, ffn_cols)] * 3,
            full(rows, cols),
            full(rows, cols),
            full(*kv_grad.shape),
            jax.ShapeDtypeStruct(mixed.shape, jnp.bfloat16),
            jax.ShapeDtypeStruct(mixed.shape, jnp.bfloat16),
        ),
        in_specs=[
            pl.BlockSpec((3, 1, 1, 80, units), lambda index: (0, 0, 0, index, 0)),
            pl.BlockSpec((3, z_size, 80, units), lambda index: (0, 0, index, 0)),
            *specs,
        ],
        out_specs=(*[row(80, ffn_cols)] * 3, *specs),
        compiler_params=pltpu.CompilerParams(vmem_limit_bytes=VMEM_BYTES),
    )(ffn_sums, ffn_grads, query_grad, out_grad, kv_grad, mixed, tokens_grad)


FF_SPLIT = 4


def ffn_pass(normed, grad_out, gate_weight, up_weight, down_weight):
    gate = jnp.dot(normed, gate_weight, preferred_element_type=jnp.float32)
    up_proj = jnp.dot(normed, up_weight, preferred_element_type=jnp.float32)
    grad_hidden = jnp.dot(grad_out, down_weight, preferred_element_type=jnp.float32)
    product, pull = jax.vjp(gelu_product, gate, up_proj)
    hidden = product.astype(jnp.bfloat16)
    grad_gate_f, grad_up_f = pull(grad_hidden)
    grad_gate = grad_gate_f.astype(jnp.bfloat16)
    grad_up = grad_up_f.astype(jnp.bfloat16)
    mixed_part = matmul_nt(hidden, down_weight).astype(jnp.bfloat16)
    normed_part = (matmul_nt(grad_gate, gate_weight) + matmul_nt(grad_up, up_weight)).astype(
        jnp.bfloat16
    )
    weight_parts = [
        matmul_tn(normed, grad_gate).astype(jnp.bfloat16),
        matmul_tn(normed, grad_up).astype(jnp.bfloat16),
        matmul_tn(grad_out, hidden).astype(jnp.bfloat16),
    ]
    return mixed_part, normed_part, weight_parts


def shards_general(
    tokens,
    segments,
    positions,
    cotangent,
    attn_gain,
    ffn_gain,
    w_kv,
    w_query,
    w_out,
    w_gate,
    w_up,
    w_down,
):
    everywhere = ("z", "xc", "mp")
    dp = ("z", "xc")
    z_size = lax.axis_size("z")
    xc_size = lax.axis_size("xc")
    gains = lax.all_gather(
        jnp.stack([attn_gain, ffn_gain], axis=1), everywhere, axis=0, tiled=True
    ).astype(jnp.float32)
    gain_one, gain_two = gains[:, 0], gains[:, 1]
    kv_weight = lax.all_gather(w_kv, everywhere, axis=0, tiled=True)
    head_dim = kv_weight.shape[1] // 2
    width = tokens.shape[1]
    seq_len = segments.shape[0]
    heads_here = w_query.shape[1] // head_dim
    scale = head_dim ** (-0.5)
    cosine, sine = rotary_angles(positions, head_dim)
    inputs_f = tokens.astype(jnp.float32)
    tokens_all = lax.all_gather(tokens, "mp", axis=0, tiled=True)
    normed_one = norm_gain(tokens_all.astype(jnp.float32), gain_one).astype(jnp.bfloat16)
    query_weight = lax.all_gather(w_query, dp, axis=0, tiled=True)
    out_weight = lax.all_gather(w_out, dp, axis=0, tiled=True)

    rows = w_gate.shape[0]
    unit = w_gate.shape[1] // z_size

    def spread(weight):
        pieces = weight.reshape(rows, z_size, unit).transpose(1, 0, 2)
        pieces = lax.all_to_all(pieces, "z", split_axis=0, concat_axis=0, tiled=True)
        return lax.all_gather(pieces, "xc", axis=1, tiled=False).reshape(width, unit)

    gate_weight, up_weight, down_weight = spread(w_gate), spread(w_up), spread(w_down)
    grad_all = lax.all_gather(cotangent, ("z", "mp"), axis=0, tiled=True)

    query = jnp.dot(normed_one, query_weight, preferred_element_type=jnp.float32).reshape(
        seq_len, heads_here, head_dim
    )
    rotated = (rotate(query, cosine[:, None], sine[:, None]) * scale).astype(jnp.bfloat16)
    keyval = jnp.dot(normed_one, kv_weight, preferred_element_type=jnp.float32)
    keys = rotate(keyval[:, :head_dim], cosine, sine).astype(jnp.bfloat16)
    values = keyval[:, head_dim:].astype(jnp.bfloat16)
    allowed = block_allowed(segments, 0, seq_len)
    scores = jnp.einsum("thd,sd->hts", rotated, keys, preferred_element_type=jnp.float32)
    scores = jnp.where(allowed[None], scores, masked_score)
    row_max = jnp.max(scores, axis=-1, keepdims=True)
    weights = jnp.exp(scores - row_max)
    probs = weights / jnp.sum(weights, axis=-1, keepdims=True)
    probs_low = probs.astype(jnp.bfloat16)
    attn_vals = (
        jnp.einsum("hts,sd->thd", probs_low, values, preferred_element_type=jnp.float32)
        .reshape(seq_len, heads_here * head_dim)
        .astype(jnp.bfloat16)
    )
    mid = inputs_f + lax.psum_scatter(
        matmul_nt(attn_vals, out_weight).astype(jnp.bfloat16),
        "mp",
        scatter_dimension=0,
        tiled=True,
    ).astype(jnp.float32)
    normed_two = norm_gain(mid, gain_two).astype(jnp.bfloat16)
    normed_all = lax.all_gather(normed_two, ("z", "mp"), axis=0, tiled=True)

    mixed_part, normed_part, weight_parts = ffn_pass(
        normed_all, grad_all, gate_weight, up_weight, down_weight
    )
    grad_normed_two = lax.psum_scatter(
        normed_part, ("z", "mp"), scatter_dimension=0, tiled=True
    ).astype(jnp.float32)
    mixed = (
        mid
        + lax.psum_scatter(mixed_part, ("z", "mp"), scatter_dimension=0, tiled=True).astype(
            jnp.float32
        )
    ).astype(jnp.bfloat16)

    def collect(part):
        pieces = part.reshape(z_size, xc_size, rows, unit).transpose(1, 0, 2, 3)
        pieces = pieces.reshape(xc_size * z_size * rows, unit)
        pieces = lax.psum_scatter(pieces, "xc", scatter_dimension=0, tiled=True)
        pieces = pieces.reshape(z_size, rows, unit)
        pieces = lax.all_to_all(pieces, "z", split_axis=0, concat_axis=0, tiled=True)
        return pieces.transpose(1, 0, 2).reshape(rows, z_size * unit).astype(jnp.float32)

    w_gate_grad, w_up_grad, w_down_grad = [collect(part) for part in weight_parts]

    norm_pull_two = jax.vjp(norm_gain, mid, gain_two)[1]
    grad_mid_norm, grad_gain_two = norm_pull_two(grad_normed_two)
    grad_mid = cotangent.astype(jnp.float32) + grad_mid_norm
    grad_mid_all = lax.all_gather(grad_mid.astype(jnp.bfloat16), "mp", axis=0, tiled=True)
    grad_vals = (
        jnp.dot(grad_mid_all, out_weight, preferred_element_type=jnp.float32)
        .astype(jnp.bfloat16)
        .reshape(seq_len, heads_here, head_dim)
    )
    grad_probs = jnp.einsum("thd,sd->hts", grad_vals, values, preferred_element_type=jnp.float32)
    delta = jnp.sum(probs * grad_probs, axis=-1, keepdims=True)
    grad_scores = (probs * (grad_probs - delta)).astype(jnp.bfloat16)
    grad_rot = jnp.einsum("hts,sd->thd", grad_scores, keys, preferred_element_type=jnp.float32)
    key_sum = jnp.einsum("hts,thd->sd", grad_scores, rotated, preferred_element_type=jnp.float32)
    value_sum = jnp.einsum("hts,thd->sd", probs_low, grad_vals, preferred_element_type=jnp.float32)
    grad_query = (
        (unrotate(grad_rot, cosine[:, None], sine[:, None]) * scale)
        .reshape(seq_len, heads_here * head_dim)
        .astype(jnp.bfloat16)
    )
    grad_kv = jnp.concatenate([unrotate(key_sum, cosine, sine), value_sum], axis=1).astype(
        jnp.bfloat16
    )
    grad_normed_one = lax.psum_scatter(
        (matmul_nt(grad_query, query_weight) + matmul_nt(grad_kv, kv_weight)).astype(jnp.bfloat16),
        "mp",
        scatter_dimension=0,
        tiled=True,
    ).astype(jnp.float32)
    norm_pull_one = jax.vjp(norm_gain, inputs_f, gain_one)[1]
    grad_input_norm, grad_gain_one = norm_pull_one(grad_normed_one)
    tokens_grad = (grad_mid + grad_input_norm).astype(jnp.bfloat16)

    w_query_grad = lax.psum_scatter(
        matmul_tn(normed_one, grad_query).astype(jnp.bfloat16), dp, scatter_dimension=0, tiled=True
    ).astype(jnp.float32)
    w_out_grad = lax.psum_scatter(
        matmul_tn(grad_mid_all, attn_vals).astype(jnp.bfloat16), dp, scatter_dimension=0, tiled=True
    ).astype(jnp.float32)
    small = jnp.concatenate(
        [matmul_tn(normed_one, grad_kv), grad_gain_one[:, None], grad_gain_two[:, None]], axis=1
    )
    small = lax.psum_scatter(small, everywhere, scatter_dimension=0, tiled=True)
    kv_grad = small[:, : 2 * head_dim]
    return (
        mixed,
        tokens_grad,
        small[:, 2 * head_dim],
        small[:, 2 * head_dim + 1],
        kv_grad,
        w_query_grad,
        w_out_grad,
        w_gate_grad,
        w_up_grad,
        w_down_grad,
    )


def shards_fast(
    tokens,
    segments,
    positions,
    cotangent,
    attn_gain,
    ffn_gain,
    w_kv,
    w_query,
    w_out,
    w_gate,
    w_up,
    w_down,
):
    quarter = w_kv.shape[1] // 8
    lane = jnp.arange(2 * quarter)
    freqs = rope_base ** (-(lane % quarter).astype(jnp.float32) / quarter)
    phase = positions.astype(jnp.float32)[:, None] * freqs[None, :]
    table = (jnp.cos(phase), jnp.where(lane < quarter, -1.0, 1.0)[None, :] * jnp.sin(phase))
    (
        normed_one,
        rotated,
        keys,
        values,
        attn_vals,
        mid,
        normed_two,
        gains,
        allowed,
        kv_weight,
        query_weight,
        out_weight,
        ffn_weights,
        grad_all,
    ) = pre_call(
        tokens,
        w_kv,
        attn_gain[None, :],
        ffn_gain[None, :],
        table,
        segments[None, :],
        cotangent,
        w_query,
        w_out,
        (w_gate, w_up, w_down),
    )
    main = ragged_split(w_gate.shape[1], lax.axis_size("z"))[0]
    grad_mid, gain_part, mix_parts, ffn_sums, grad_mid_low = ffn_call(
        gains, normed_two, grad_all, ffn_weights, mid, w_gate.shape[0], main
    )
    mixed, tokens_grad, gain_grads, kv_grad, query_grad, out_grad, ffn_grads = post_call(
        tokens,
        gains,
        gain_part,
        normed_one,
        rotated,
        keys,
        values,
        attn_vals,
        table,
        allowed,
        kv_weight,
        query_weight,
        out_weight,
        mix_parts,
        grad_mid,
        grad_mid_low,
        mid,
        ffn_sums,
        main,
    )
    *ffn_out, query_grad, out_grad, kv_grad, mixed, tokens_grad = layout_call(
        ffn_sums,
        ffn_grads,
        query_grad,
        out_grad,
        kv_grad,
        mixed,
        tokens_grad,
        w_gate.shape[1],
    )
    share = attn_gain.shape[0]
    place = lax.axis_index(("z", "x", "c", "mp")) * share
    gain_grads = gain_grads.reshape(2, gain_grads.size // 2)
    gain_grads = lax.dynamic_slice(gain_grads, (0, place), (2, share))
    return (
        mixed,
        tokens_grad,
        gain_grads[0],
        gain_grads[1],
        kv_grad,
        query_grad,
        out_grad,
        *ffn_out,
    )


def solution(mesh):
    dp_size, mp_size = mesh.shape["dp"], mesh.shape["mp"]
    if dp_size == 4 * FF_SPLIT and mp_size == 2:
        body, dp = shards_fast, ("z", "x", "c")
        sizes = (FF_SPLIT, 2, 2, mp_size)
    else:
        body, dp = shards_general, ("z", "xc")
        sizes = (FF_SPLIT, dp_size // FF_SPLIT, mp_size)
    all_axes = (*dp, "mp")
    fine = jax.sharding.Mesh(mesh.devices.reshape(sizes), all_axes)
    in_specs = (
        P(all_axes, None),
        P(dp),
        P(dp),
        P(all_axes, None),
        P(all_axes),
        P(all_axes),
        P(all_axes, None),
        P(dp, "mp"),
        P(dp, "mp"),
        P(dp, "mp"),
        P(dp, "mp"),
        P(dp, "mp"),
    )
    out_specs = (
        P(all_axes, None),
        P(all_axes, None),
        P(all_axes),
        P(all_axes),
        P(all_axes, None),
        P(dp, "mp"),
        P(dp, "mp"),
        P(dp, "mp"),
        P(dp, "mp"),
        P(dp, "mp"),
    )
    return jax.shard_map(body, mesh=fine, in_specs=in_specs, out_specs=out_specs, check_vma=False)
```

```python
import functools

import jax
import jax.numpy as jnp
from jax import lax
from jax.experimental import pallas as pl
from jax.experimental.pallas import tpu as pltpu
from jax.sharding import PartitionSpec as P

WINDOW = 2048


epsilon = 1e-06
rope_base = 10000.0
masked_score = -1e30
VMEM_BYTES = 66_000_000


def norm_gain(values, gain):
    return values * lax.rsqrt(jnp.mean(values * values, axis=-1, keepdims=True) + epsilon) * gain


def rotary_angles(positions, head_width):
    quarter = head_width // 4
    freqs = rope_base ** (-jnp.arange(quarter).astype(jnp.float32) / quarter)
    phase = positions.astype(jnp.float32)[:, None] * freqs[None, :]
    return (jnp.cos(phase), jnp.sin(phase))


def rotate(values, cosine, sine):
    quarter = cosine.shape[-1]
    first_half = values[..., :quarter]
    second_half = values[..., quarter : 2 * quarter]
    return jnp.concatenate(
        [
            first_half * cosine - second_half * sine,
            second_half * cosine + first_half * sine,
            values[..., 2 * quarter :],
        ],
        axis=-1,
    )


def unrotate(values, cosine, sine):
    quarter = cosine.shape[-1]
    first_half = values[..., :quarter]
    second_half = values[..., quarter : 2 * quarter]
    return jnp.concatenate(
        [
            first_half * cosine + second_half * sine,
            second_half * cosine - first_half * sine,
            values[..., 2 * quarter :],
        ],
        axis=-1,
    )


def gelu_product(gate, up_proj):
    return jax.nn.gelu(gate, approximate=True) * up_proj


def matmul_nt(left, right):
    return lax.dot_general(
        left, right, (((1,), (1,)), ((), ())), preferred_element_type=jnp.float32
    )


def matmul_tn(left, right):
    return lax.dot_general(
        left, right, (((0,), (0,)), ((), ())), preferred_element_type=jnp.float32
    )


def block_allowed(segments, first_row, rows):
    seq_len = segments.shape[0]
    query_rows = first_row + jnp.arange(rows)
    key_rows = jnp.arange(seq_len)
    return (
        (segments[:, None] == segments[None, :])
        & (key_rows[None, :] <= query_rows[:, None])
        & (query_rows[:, None] - key_rows[None, :] < WINDOW)
    )


MESH_ID = pl.DeviceIdType.MESH
GELU_A = 0.7978845608028654
GELU_B = 0.044715
TILE = 256
WIDE = 512


def remote(src, dst, send_sem, recv_sem, where):
    return pltpu.make_async_remote_copy(
        src_ref=src,
        dst_ref=dst,
        send_sem=send_sem,
        recv_sem=recv_sem,
        device_id=where,
        device_id_type=MESH_ID,
    )


class Halves:
    def __init__(self, src, dst, send_sem, recv_sem, where):
        rows = src.shape[0] // 2
        cuts = [pl.ds(part * rows, rows) for part in range(2)]
        self.copies = [
            remote(src.at[cut], dst.at[cut], send_sem.at[part], recv_sem.at[part], where)
            for part, cut in enumerate(cuts)
        ]

    def start(self):
        for copy in self.copies:
            copy.start()

    def wait_recv(self):
        for copy in self.copies:
            copy.wait_recv()

    def wait_send(self):
        for copy in self.copies:
            copy.wait_send()


def dot_nn(left, right):
    return lax.dot_general(
        left, right, (((1,), (0,)), ((), ())), preferred_element_type=jnp.float32
    )


def gelu_parts(gate):
    square = gate * gate
    bend = jnp.tanh(GELU_A * gate * (1.0 + GELU_B * square))
    half = 0.5 * (1.0 + bend)
    slope = half + 0.5 * gate * (1.0 - bend * bend) * GELU_A * (1.0 + 3.0 * GELU_B * square)
    return gate * half, slope


def add_rows(first, rest, out, count):
    def body(index, carry):
        step = pl.ds(pl.multiple_of(index * 32, 32), 32)
        total = first[step, :].astype(jnp.float32)
        for other in rest:
            total = total + other[step, :].astype(jnp.float32)
        out[step, :] = total.astype(out.dtype)
        return carry

    lax.fori_loop(0, count // 32, body, 0)


def norm_back(values, gain, upstream):
    scale = lax.rsqrt(jnp.mean(values * values, axis=-1, keepdims=True) + epsilon)
    normed = values * scale
    pulled = gain * upstream
    back = scale * (pulled - normed * jnp.mean(normed * pulled, axis=-1, keepdims=True))
    return back, jnp.sum(upstream * normed, axis=0, keepdims=True)


def ffn_kernel(
    z_size,
    main,
    gain_ref,
    own_hbm,
    dy_hbm,
    w_hbm,
    mid_hbm,
    gm_ref,
    gain_part,
    mix_hbm,
    sums_hbm,
    gm_hbm,
    n2,
    dy,
    w3,
    h3,
    n2_t,
    dy_t,
    gn_part,
    mix_buf,
    gn_y,
    gn_z,
    gn_s,
    c_in,
    x_in,
    mid,
    load_sem,
    mix_sem,
    ag_y_send,
    ag_y_recv,
    ag_z_send,
    ag_z_recv,
    rs_y_send,
    rs_y_recv,
    rs_z_send,
    rs_z_recv,
    c_send,
    c_recv,
    x_send,
    x_recv,
    out_sem,
):
    own = own_hbm.shape[0] // 2
    width = own_hbm.shape[1]
    units = w3.shape[2]
    rows = c_in.shape[3]
    span = width // z_size
    me_y, me_z = lax.axis_index("mp"), lax.axis_index("z")
    me_x, me_c = lax.axis_index("x"), lax.axis_index("c")
    mine = pl.ds(pl.multiple_of(me_y * own, own), own)
    theirs = pl.ds(pl.multiple_of((1 - me_y) * own, own), own)
    to_y, to_x, to_c = {"mp": 1 - me_y}, {"x": 1 - me_x}, {"c": 1 - me_c}

    def ahead(step):
        return lax.rem(me_z + step, z_size)

    def to_z(step):
        return {"z": ahead(step)}

    def row_block(z_at, x_at, c_at):
        return pl.ds(pl.multiple_of(((z_at * 2 + x_at) * 2 + c_at) * rows, rows), rows)

    inner = (me_z > 0) & (me_z < z_size - 1)
    outer = (me_z == 0) | (me_z == z_size - 1)

    def w_load(index, columns):
        cols = pl.ds(0, columns)
        return pltpu.make_async_copy(
            w_hbm.at[index, :, cols], w3.at[index, :, cols], load_sem.at[z_size + index]
        )

    def w_loads(act):
        for case, columns in ((inner, units), (outer, main)):

            @pl.when(case)
            def _(columns=columns):
                for index in range(3):
                    act(w_load(index, columns))

    w_loads(lambda copy: copy.start())
    dy_loads = [
        pltpu.make_async_copy(dy_hbm.at[index], dy, load_sem.at[index])
        for index in range(z_size)
    ]
    own_load = pltpu.make_async_copy(own_hbm, n2.at[0], load_sem.at[z_size + 3])
    mid_load = pltpu.make_async_copy(mid_hbm, mid, load_sem.at[z_size + 4])
    for load in (own_load, dy_loads[0], mid_load):
        load.start()

    barrier = pltpu.get_barrier_semaphore()
    peers = [to_y, to_x, to_c] + [to_z(step) for step in range(1, z_size)]
    for where in peers:
        pl.semaphore_signal(barrier, inc=1, device_id=where, device_id_type=MESH_ID)
    pl.semaphore_wait(barrier, len(peers))

    def ag_y(index):
        block = n2.at[index, mine]
        return Halves(block, block, ag_y_send.at[index], ag_y_recv.at[index], to_y)

    def ag_y_in(index):
        block = n2.at[index, theirs]
        return Halves(block, block, ag_y_send.at[index], ag_y_recv.at[index], to_y)

    def ag_z(index):
        src = own_hbm.at[mine] if index == 0 else n2.at[index, mine]
        return Halves(
            src, n2.at[index + 1, mine], ag_z_send.at[index], ag_z_recv.at[index + 1], to_z(1)
        )

    def ag_z_in(index):
        block = n2.at[index, mine]
        return Halves(block, block, ag_z_send.at[0], ag_z_recv.at[index], to_z(1))

    def ag_last():
        return Halves(
            n2.at[2, theirs], n2.at[3, theirs], ag_y_send.at[3], ag_y_recv.at[3], to_z(1)
        )

    def forward(index):
        ag_z_in(index).wait_recv()
        ag_z(index).start()
        ag_y(index).start()

    ag_z(0).start()

    mix_copies = []

    def turn(source, target, index):
        def turn_tile(tile, carry):
            at = pl.ds(pl.multiple_of(tile * span, 128), span)
            target[at, pl.ds(index * 2 * own, 2 * own)] = source[:, at].T
            return carry

        lax.fori_loop(0, z_size, turn_tile, 0)

    def chunk(index):
        if index:
            mix_copies[index - 1].wait()
        dy_loads[index].wait()
        rows_at = pl.ds(index * 2 * own, 2 * own)

        def up_tile(tile, carry):
            cols = pl.ds(pl.multiple_of(tile * WIDE, WIDE), WIDE)
            gate = dot_nn(n2[index], w3[0, :, cols])
            up_proj = dot_nn(n2[index], w3[1, :, cols])
            grad_hidden = dot_nn(dy[...], w3[2, :, cols])
            act, slope = gelu_parts(gate)
            h3[0, rows_at, cols] = (grad_hidden * up_proj * slope).astype(jnp.bfloat16)
            h3[1, rows_at, cols] = (grad_hidden * act).astype(jnp.bfloat16)
            h3[2, rows_at, cols] = (act * up_proj).astype(jnp.bfloat16)
            return carry

        lax.fori_loop(0, units // WIDE, up_tile, 0)

        def down_tile(tile, carry):
            at = pl.ds(pl.multiple_of(tile * span, 128), span)
            normed = matmul_nt(w3[0, at, :], h3[0, rows_at, :]) + matmul_nt(
                w3[1, at, :], h3[1, rows_at, :]
            )
            mixed = matmul_nt(w3[2, at, :], h3[2, rows_at, :])
            for half in range(2):
                cols = slice(half * own, (half + 1) * own)
                gn_part[index, half, at, :] = normed[:, cols].astype(jnp.bfloat16)
                mix_buf[half, at, :] = mixed[:, cols].astype(jnp.bfloat16)
            return carry

        lax.fori_loop(0, z_size, down_tile, 0)
        copy = pltpu.make_async_copy(mix_buf, mix_hbm.at[index], mix_sem.at[index])
        copy.start()
        mix_copies.append(copy)
        if index:
            rs_y(index).start()
        turn(n2.at[index], n2_t, index)
        turn(dy, dy_t, index)
        if index + 1 < z_size:
            dy_loads[index + 1].start()

    def rs_y(index):
        return Halves(
            gn_part.at[index, 1 - me_y], gn_y.at[index], rs_y_send.at[index], rs_y_recv.at[index], to_y
        )

    def rs_z(index):
        return Halves(
            gn_s.at[index - 1],
            gn_z.at[index - 1],
            rs_z_send.at[index],
            rs_z_recv.at[index - 1],
            to_z(1),
        )

    def rs_step(index):
        rs_y(index).wait_recv()
        slot = (index - 2) % z_size
        if index != 1:
            Halves(
                gn_s.at[slot], gn_z.at[slot], rs_z_send.at[1], rs_z_recv.at[slot], to_z(1)
            ).wait_recv()

        def add_tile(tile, carry):
            at = pl.ds(pl.multiple_of(tile * TILE, TILE), TILE)
            total = gn_part[index, me_y, at, :].astype(jnp.float32) + gn_y[index, at, :].astype(
                jnp.float32
            )
            if index != 1:
                total = total + gn_z[slot, at, :].astype(jnp.float32)
            if index == 0:
                gm_ref[:, at] = total.T
            else:
                gn_s[index - 1, at, :] = total.astype(jnp.bfloat16)
            return carry

        lax.fori_loop(0, width // TILE, add_tile, 0)
        if index != 0:
            rs_z(index).start()


    def grads(step):
        at = pl.ds(pl.multiple_of(ahead(step) * span, 128), span)
        for kind, source in enumerate((n2_t, n2_t, dy_t)):

            def tile_body(tile, carry, kind=kind, source=source):
                cols = pl.ds(pl.multiple_of(tile * WIDE, WIDE), WIDE)
                w3[kind, at, cols] = dot_nn(source[at, :], h3[kind, :, cols]).astype(jnp.bfloat16)
                return carry

            lax.fori_loop(0, units // WIDE, tile_body, 0)
            for far in (1, 0):
                over_c(kind, step, far).start()

    def over_c(kind, step, far):
        x_at = 1 - me_x if far else me_x
        return remote(
            w3.at[kind, row_block(ahead(step), x_at, 1 - me_c)],
            c_in.at[kind, step, far],
            c_send.at[kind, step, far],
            c_recv.at[kind, step, far],
            to_c,
        )

    def over_x(kind):
        return remote(
            w3.at[kind, row_block(ahead(1), 1 - me_x, me_c)],
            x_in.at[kind],
            x_send.at[kind],
            x_recv.at[kind],
            to_x,
        )

    out_copies = []

    def keep(kind, step, far, block):
        copy = pltpu.make_async_copy(
            block, sums_hbm.at[kind, step, far], out_sem.at[kind, step, far]
        )
        copy.start()
        out_copies.append(copy)

    def core_sums(step):
        pairs = [(kind, far) for kind in range(3) for far in (1, 0)]
        if step == 1:
            pairs.sort(key=lambda pair: -pair[1])
        for kind, far in pairs:
            over_c(kind, step, far).wait_recv()
            x_at = 1 - me_x if far else me_x
            block = w3.at[kind, row_block(ahead(step), x_at, me_c)]
            add_rows(block, [c_in.at[kind, step, far]], block, rows)
            if step != 1:
                keep(kind, step, far, block)
            elif far:
                over_x(kind).start()

    def first_sums():
        for kind in range(3):
            over_x(kind).wait_recv()
            block = w3.at[kind, row_block(ahead(1), me_x, me_c)]
            add_rows(block, [x_in.at[kind]], block, rows)
            keep(kind, 1, 0, block)

    own_load.wait()
    w_loads(lambda copy: copy.wait())

    @pl.when(outer)
    def _():
        w3[:, :, main:] = jnp.zeros((3, width, units - main), jnp.bfloat16)

    chunk(0)
    forward(1)
    forward(2)
    ag_y_in(1).wait_recv()
    chunk(1)
    ag_y_in(2).wait_recv()
    ag_last().start()
    chunk(2)
    rs_step(1)
    ag_z_in(3).wait_recv()
    ag_last().wait_recv()
    chunk(3)
    rs_y(0).start()
    rs_step(2)
    grads(1)
    grads(2)
    core_sums(1)
    rs_step(3)
    grads(3)
    core_sums(2)
    grads(0)
    core_sums(3)
    rs_step(0)
    core_sums(0)

    cot_load = pltpu.make_async_copy(
        dy_hbm.at[0, mine], dy.at[pl.ds(0, own)], load_sem.at[z_size + 3]
    )
    cot_load.start()
    cot_load.wait()
    mid_load.wait()

    def mid_rows(index, total):
        at = pl.ds(pl.multiple_of(index * 32, 32), 32)
        grad, gain_sum = norm_back(mid[at, :], gain_ref[1:2, :], gm_ref[at, :])
        grad = grad + dy[at, :].astype(jnp.float32)
        gm_ref[at, :] = grad
        dy[pl.ds(pl.multiple_of(own + index * 32, 32), 32), :] = grad.astype(jnp.bfloat16)
        return total + gain_sum

    gain_sum = lax.fori_loop(0, own // 32, mid_rows, jnp.zeros((1, width), jnp.float32))
    gm_save = pltpu.make_async_copy(dy.at[pl.ds(own, own)], gm_hbm, load_sem.at[z_size + 3])
    gm_save.start()
    for index in range(4):
        gain_part[index : index + 1, :] = jnp.zeros((1, span), jnp.float32)
        gain_part[4 + index : 5 + index, :] = gain_sum[:, index * span : (index + 1) * span]
    first_sums()
    gm_save.wait()

    for copy in mix_copies[3:] + out_copies:
        copy.wait()
    for index in range(z_size):
        if index in (1, 2):
            ag_y(index).wait_send()
        if index == 3:
            ag_last().wait_send()
        rs_y(index).wait_send()
        if index < z_size - 1:
            ag_z(index).wait_send()
        if index:
            rs_z(index).wait_send()
        for kind in range(3):
            over_c(kind, index, 0).wait_send()
            over_c(kind, index, 1).wait_send()
            if index == 1:
                over_x(kind).wait_send()


def ffn_call(gains, normed, grad_all, weights, mid, rows, main):
    z_size = lax.axis_size("z")
    pair, width = normed.shape
    units = weights.shape[2]
    own = pair // 2
    wide = lambda *lead: pltpu.VMEM((*lead, width), jnp.bfloat16)
    tall = lambda *lead: pltpu.VMEM((*lead, width, own), jnp.bfloat16)
    dma = lambda *lead: pltpu.SemaphoreType.DMA(lead)
    vmem = pl.BlockSpec(memory_space=pltpu.VMEM)
    hbm = pl.BlockSpec(memory_space=pl.ANY)
    return pl.pallas_call(
        functools.partial(ffn_kernel, z_size, main),
        out_shape=(
            jax.ShapeDtypeStruct((own, width), jnp.float32),
            jax.ShapeDtypeStruct((8, width // z_size), jnp.float32),
            jax.ShapeDtypeStruct((z_size, 2, width, own), jnp.bfloat16),
            jax.ShapeDtypeStruct((3, z_size, 2, rows, units), jnp.bfloat16),
            jax.ShapeDtypeStruct((own, width), jnp.bfloat16),
        ),
        in_specs=[vmem, hbm, hbm, hbm, hbm],
        out_specs=(vmem, vmem, hbm, hbm, hbm),
        scratch_shapes=[
            wide(z_size, pair),
            wide(pair),
            pltpu.VMEM(weights.shape, jnp.bfloat16),
            pltpu.VMEM((3, z_size * pair, units), jnp.bfloat16),
            pltpu.VMEM((width, z_size * pair), jnp.bfloat16),
            pltpu.VMEM((width, z_size * pair), jnp.bfloat16),
            tall(z_size, 2),
            tall(2),
            tall(z_size),
            tall(z_size - 1),
            tall(z_size - 1),
            pltpu.VMEM((3, z_size, 2, rows, units), jnp.bfloat16),
            pltpu.VMEM((3, rows, units), jnp.bfloat16),
            pltpu.VMEM((own, width), jnp.float32),
            dma(z_size + 5),
            dma(z_size),
            dma(z_size, 2),
            dma(z_size, 2),
            dma(z_size, 2),
            dma(z_size, 2),
            dma(z_size, 2),
            dma(z_size, 2),
            dma(z_size, 2),
            dma(z_size, 2),
            dma(3, z_size, 2),
            dma(3, z_size, 2),
            dma(3),
            dma(3),
            dma(3, z_size, 2),
        ],
        compiler_params=pltpu.CompilerParams(
            collective_id=0, has_side_effects=True, vmem_limit_bytes=VMEM_BYTES
        ),
        cost_estimate=pl.CostEstimate(
            flops=18 * z_size * pair * width * units,
            bytes_accessed=4 * weights.size + 12 * z_size * pair * width,
            transcendentals=z_size * pair * units,
        ),
    )(gains, normed, grad_all, weights, mid)


def spin(values, table):
    first = values[:, : values.shape[1] // 2]
    turned = first * table[0] + pltpu.roll(first, first.shape[1] // 2, 1) * table[1]
    return jnp.concatenate([turned, values[:, values.shape[1] // 2 :]], axis=1)


def spin_back(values, table):
    first = values[:, : values.shape[1] // 2]
    turned = first * table[0] - pltpu.roll(first, first.shape[1] // 2, 1) * table[1]
    return jnp.concatenate([turned, values[:, values.shape[1] // 2 :]], axis=1)


def head_probs(rotated, keys, allowed):
    scores = jnp.where(allowed > 0.5, matmul_nt(rotated, keys), masked_score)
    weights = jnp.exp(scores - jnp.max(scores, axis=-1, keepdims=True))
    return weights / jnp.sum(weights, axis=-1, keepdims=True)


def ragged_split(columns, parts):
    main = columns // parts // 128 * 128
    return main, main + 128


def pre_kernel(
    z_size,
    tok_ref,
    wkv_ref,
    gain_one_ref,
    gain_two_ref,
    cos_ref,
    sin_ref,
    seg_ref,
    cot_hbm,
    wq_hbm,
    wo_hbm,
    wg_hbm,
    wu_hbm,
    wd_hbm,
    n1_ref,
    rot_ref,
    key_ref,
    val_ref,
    att_ref,
    mid_ref,
    n2_ref,
    gain_ref,
    allow_ref,
    kv_out,
    wq_out,
    wo_out,
    w3_out,
    dy_out,
    kv_w,
    q_w,
    o_w,
    tok,
    part,
    part_y,
    query,
    gain_rows,
    y_send,
    y_recv,
    ky_send,
    ky_recv,
    az_send,
    az_recv,
    ax_send,
    ax_recv,
    ac_send,
    ac_recv,
    fz_send,
    fz_recv,
    fx_send,
    fx_recv,
    fc_send,
    fc_recv,
    dz_send,
    dz_recv,
    dy_send,
    dy_recv,
    local_sem,
):
    me_z, me_x = lax.axis_index("z"), lax.axis_index("x")
    me_c, me_y = lax.axis_index("c"), lax.axis_index("mp")
    own, width = tok_ref.shape
    rows = wq_hbm.shape[0]
    half_rows = wkv_ref.shape[0]
    head = key_ref.shape[1]
    main, units = ragged_split(wg_hbm.shape[1], z_size)
    to_y, to_x, to_c = {"mp": 1 - me_y}, {"x": 1 - me_x}, {"c": 1 - me_c}

    def to_z(step):
        return {"z": lax.rem(me_z + step, z_size)}

    def from_z(step):
        return lax.rem(me_z - step + z_size, z_size)

    def row_block(step, x_at, c_at):
        start = ((from_z(step) * 2 + x_at) * 2 + c_at) * rows
        return pl.ds(pl.multiple_of(start, rows), rows)

    mine = pl.ds(pl.multiple_of(me_y * own, own), own)
    theirs = pl.ds(pl.multiple_of((1 - me_y) * own, own), own)
    bufs = (kv_w, q_w, o_w)
    inputs = (None, wq_hbm, wo_hbm)

    locals_ = []

    def local(src, dst):
        copy = pltpu.make_async_copy(src, dst, local_sem.at[len(locals_)])
        copy.start()
        locals_.append(copy)
        return copy

    here = row_block(0, me_x, me_c)
    own_q = local(wq_hbm, q_w.at[here])
    own_o = local(wo_hbm, o_w.at[here])
    ffn_in = (wg_hbm, wu_hbm, wd_hbm)

    def body_of(target):
        return pl.ds(pl.multiple_of(target * main, 128), main), pl.ds(0, main)

    def tail_of(target):
        start = z_size * main + lax.rem(target + 1, 2) * 128
        return pl.ds(pl.multiple_of(start, 128), 128), pl.ds(main, 128)

    def is_inner(at):
        return (at > 0) & (at < z_size - 1)

    own_f = []
    for kind in range(3):
        src, dst = body_of(me_z)
        own_f.append(local(ffn_in[kind].at[:, src], w3_out.at[kind, here, dst]))

    def own_tail(kind):
        src, dst = tail_of(me_z)
        return pltpu.make_async_copy(
            ffn_in[kind].at[:, src], w3_out.at[kind, here, dst], local_sem.at[12 + kind]
        )

    @pl.when(is_inner(me_z))
    def _():
        for kind in range(3):
            own_tail(kind).start()
    own_d = local(cot_hbm, dy_out.at[0, mine])

    kv_own = pl.ds(pl.multiple_of(here.start + me_y * half_rows, half_rows), half_rows)
    gain_rows[...] = jnp.zeros(gain_rows.shape, jnp.float32)
    gain_rows[0:1, :half_rows] = gain_one_ref[...].astype(jnp.float32)
    gain_rows[1:2, :half_rows] = gain_two_ref[...].astype(jnp.float32)
    spread = gain_rows[...].T
    kv_w[kv_own, : 2 * head] = wkv_ref[...]
    kv_w[kv_own, 2 * head :] = spread[:half_rows, :].astype(jnp.bfloat16)

    barrier = pltpu.get_barrier_semaphore()
    peers = [to_y, to_x, to_c] + [to_z(step) for step in range(1, z_size)]
    for where in peers:
        pl.semaphore_signal(barrier, inc=1, device_id=where, device_id_type=MESH_ID)
    pl.semaphore_wait(barrier, len(peers))

    tok_y = remote(tok_ref, tok.at[mine], y_send.at[1], y_recv.at[1], to_y)
    tok_y_in = remote(tok_ref, tok.at[theirs], y_send.at[1], y_recv.at[1], to_y)
    part_out = remote(part.at[theirs], part_y, y_send.at[2], y_recv.at[2], to_y)
    n2_y = remote(n2_ref.at[mine], n2_ref.at[mine], y_send.at[3], y_recv.at[3], to_y)
    n2_y_in = remote(n2_ref.at[theirs], n2_ref.at[theirs], y_send.at[3], y_recv.at[3], to_y)

    def block_of(kind, step, x_at):
        if kind:
            return row_block(step, x_at, me_c)
        return kv_rows(step, x_at, me_y)

    def kv_rows(step, x_at, y_at):
        start = row_block(step, x_at, me_c).start + y_at * half_rows
        return pl.ds(pl.multiple_of(start, half_rows), half_rows)

    def kv_y(step, far):
        x_at = 1 - me_x if far else me_x
        block = kv_w.at[kv_rows(step, x_at, me_y)]
        slot = step + z_size * far
        return remote(block, block, ky_send.at[slot], ky_recv.at[slot], to_y)

    def kv_y_in(step, far):
        x_at = 1 - me_x if far else me_x
        block = kv_w.at[kv_rows(step, x_at, 1 - me_y)]
        slot = step + z_size * far
        return remote(block, block, ky_send.at[slot], ky_recv.at[slot], to_y)

    def source(kind, step):
        if isinstance(step, int) and step == 0 and kind:
            return inputs[kind]
        return bufs[kind].at[block_of(kind, step, me_x)]

    first_z, last_z = (z_size - 1 - me_z) // (z_size - 1), me_z // (z_size - 1)
    inner = first_z + last_z == 0
    order = (0, 1 + 2 * first_z, 3 - first_z - last_z, 2 - first_z + last_z)
    hops = (
        None,
        (lax.rem(me_z + 1, z_size), 2),
        (lax.rem(me_z + z_size - 1, z_size), 2),
        (lax.rem(3 * (me_z + 3), z_size), lax.rem(2 * me_z + 3, z_size)),
    )

    def a_z_own(kind, right):
        return remote(
            source(kind, 0),
            bufs[kind].at[block_of(kind, 0, me_x)],
            az_send.at[kind, right],
            az_recv.at[kind, 1 if right else z_size - 1],
            to_z(1 if right else z_size - 1),
        )

    def a_z_start(kind):
        @pl.when(last_z == 0)
        def _():
            a_z_own(kind, 1).start()

        @pl.when(first_z == 0)
        def _():
            a_z_own(kind, 0).start()

    def a_z(kind, index):
        target, slot = hops[index]
        block = bufs[kind].at[block_of(kind, order[index], me_x)]
        return remote(
            block, block, az_send.at[kind, 1 + index], az_recv.at[kind, slot], {"z": target}
        )

    def a_z_next(kind, index):
        @pl.when(inner)
        def _():
            a_z(kind, index).start()

    def a_z_done(kind):
        @pl.when(last_z == 0)
        def _():
            a_z_own(kind, 1).wait_send()

        @pl.when(first_z == 0)
        def _():
            a_z_own(kind, 0).wait_send()

        @pl.when(inner)
        def _():
            for index in range(1, z_size):
                a_z(kind, index).wait_send()

    def a_z_in(kind, step):
        block = bufs[kind].at[block_of(kind, step, me_x)]
        return remote(block, block, az_send.at[kind, 0], az_recv.at[kind, step], to_z(1))

    def a_x(kind, step):
        return remote(
            source(kind, step),
            bufs[kind].at[block_of(kind, step, me_x)],
            ax_send.at[kind, step],
            ax_recv.at[kind, step],
            to_x,
        )

    def a_x_in(kind, step):
        block = bufs[kind].at[block_of(kind, step, 1 - me_x)]
        return remote(block, block, ax_send.at[kind, step], ax_recv.at[kind, step], to_x)

    def a_c(kind, step, far):
        x_at = 1 - me_x if far else me_x
        block = bufs[kind].at[row_block(step, x_at, me_c)]
        src = source(kind, step) if kind and not far else block
        slot = step + z_size * far
        return remote(src, block, ac_send.at[kind, slot], ac_recv.at[kind, slot], to_c)

    def a_c_in(kind, step, far):
        x_at = 1 - me_x if far else me_x
        block = bufs[kind].at[row_block(step, x_at, 1 - me_c)]
        slot = step + z_size * far
        return remote(block, block, ac_send.at[kind, slot], ac_recv.at[kind, slot], to_c)

    def f_z(kind, step, act):
        target = lax.rem(me_z + step, z_size)

        def piece(index, src, dst):
            return remote(
                ffn_in[kind].at[:, src],
                w3_out.at[kind, here, dst],
                fz_send.at[kind, step, index],
                fz_recv.at[kind, step, index],
                to_z(step),
            )

        act(piece(0, *body_of(target)))

        @pl.when(is_inner(target))
        def _():
            act(piece(1, *tail_of(target)))

    def f_z_wait(kind, step):
        block = row_block(step, me_x, me_c)

        def piece(index, dst):
            part = w3_out.at[kind, block, dst]
            return remote(
                part, part, fz_send.at[kind, step, index], fz_recv.at[kind, step, index], to_z(step)
            )

        piece(0, pl.ds(0, main)).wait_recv()

        @pl.when(inner)
        def _():
            piece(1, pl.ds(main, 128)).wait_recv()

    def f_x(kind, step, x_at, act):
        for case, columns in ((inner, units), (first_z + last_z > 0, main)):

            @pl.when(case)
            def _(columns=columns):
                block = w3_out.at[kind, row_block(step, x_at, me_c), pl.ds(0, columns)]
                act(remote(block, block, fx_send.at[kind, step], fx_recv.at[kind, step], to_x))

    def f_x_start(kind, step):
        f_x(kind, step, me_x, lambda copy: copy.start())

    def f_x_wait(kind, step):
        f_x(kind, step, 1 - me_x, lambda copy: copy.wait_recv())

    def f_x_done(kind, step):
        f_x(kind, step, me_x, lambda copy: copy.wait_send())

    def f_c(kind, step, far):
        block = w3_out.at[kind, row_block(step, 1 - me_x if far else me_x, me_c)]
        slot = step + z_size * far
        return remote(block, block, fc_send.at[kind, slot], fc_recv.at[kind, slot], to_c)

    def f_c_in(kind, step, far):
        block = w3_out.at[kind, row_block(step, 1 - me_x if far else me_x, 1 - me_c)]
        slot = step + z_size * far
        return remote(block, block, fc_send.at[kind, slot], fc_recv.at[kind, slot], to_c)

    def d_source(step):
        return cot_hbm if isinstance(step, int) else dy_out.at[step, mine]

    def d_z_own(right):
        slot = 1 if right else z_size - 1
        return remote(
            cot_hbm, dy_out.at[slot, mine], dz_send.at[right], dz_recv.at[slot], to_z(slot)
        )

    def d_z_start():
        @pl.when(last_z == 0)
        def _():
            d_z_own(1).start()

        @pl.when(first_z == 0)
        def _():
            d_z_own(0).start()

    def d_z(index):
        target, slot = hops[index]
        return remote(
            dy_out.at[order[index], mine],
            dy_out.at[slot, mine],
            dz_send.at[1 + index],
            dz_recv.at[slot],
            {"z": target},
        )

    def d_z_done():
        @pl.when(last_z == 0)
        def _():
            d_z_own(1).wait_send()

        @pl.when(first_z == 0)
        def _():
            d_z_own(0).wait_send()

        @pl.when(inner)
        def _():
            for index in range(1, z_size):
                d_z(index).wait_send()

    def d_z_in(step):
        block = dy_out.at[step, mine]
        return remote(block, block, dz_send.at[0], dz_recv.at[step], to_z(1))

    def d_y(step):
        return remote(
            d_source(step), dy_out.at[step, mine], dy_send.at[step], dy_recv.at[step], to_y
        )

    def d_y_in(step):
        block = dy_out.at[step, theirs]
        return remote(block, block, dy_send.at[step], dy_recv.at[step], to_y)

    for kind in (1, 0, 2):
        a_z_start(kind)
        a_x(kind, 0).start()
    kv_y(0, 0).start()
    tok_y.start()
    for kind in (1, 2):
        a_c(kind, 0, 0).start()

    for at_end, away in ((first_z, 1), (last_z, z_size - 1)):

        @pl.when(at_end > 0)
        def _(away=away):
            for kind in range(3):
                f_z(kind, away, lambda copy: copy.start())

    tok[mine, :] = tok_ref[...]
    seq = 2 * own
    query_at = lax.broadcasted_iota(jnp.int32, (seq, seq), 0)
    key_at = lax.broadcasted_iota(jnp.int32, (seq, seq), 1)
    segment = seg_ref[...].astype(jnp.float32)
    same = jnp.broadcast_to(segment, (8, seq)).T[:, :1] == segment
    allowed = same & (key_at <= query_at) & (query_at - key_at < WINDOW)
    allow_ref[...] = jnp.where(allowed, 1.0, 0.0)
    d_y(0).start()

    def from_x(index):
        step = order[index]
        for kind in (1, 0, 2):
            a_x_in(kind, step).wait_recv()
            if kind:
                a_c(kind, step, 1).start()
            else:
                kv_y(step, 1).start()

    def from_y(index):
        step = order[index]
        for far in range(2):
            kv_y_in(step, far).wait_recv()
            a_c(0, step, far).start()

    for index in range(1, z_size):
        step = order[index]
        for kind in (1, 0, 2):
            a_z_in(kind, step).wait_recv()
            a_z_next(kind, index)
            a_x(kind, step).start()
            if kind:
                a_c(kind, step, 0).start()
            else:
                kv_y(step, 0).start()
        if index == z_size - 2:
            d_z_start()
        if index == z_size - 1:
            for copy in own_f:
                copy.wait()

            @pl.when(inner)
            def _():
                for kind in range(3):
                    own_tail(kind).wait()

            for kind in range(3):
                for away, sent in ((1, first_z), (3, last_z), (2, 0)):

                    @pl.when(sent == 0 if away != 2 else me_z >= 0)
                    def _(kind=kind, away=away):
                        f_z(kind, away, lambda copy: copy.start())

            for kind in range(3):
                f_x_start(kind, 0)
                f_c(kind, 0, 0).start()
        if index >= 2:
            from_x(index - 2)
            from_y(index - 2)
    for index in (z_size - 2, z_size - 1):
        from_x(index)
        from_y(index)

    def hand_on(kind, step):
        f_z_wait(kind, step)
        f_x_start(kind, step)
        f_c(kind, step, 0).start()

    def cross(kind, step):
        f_x_wait(kind, step)
        f_c(kind, step, 1).start()

    def pass_cotangent(step):
        d_z_in(order[step]).wait_recv()

        @pl.when(inner)
        def _():
            d_z(step).start()

        d_y(order[step]).start()

    def pass_if(case, step):
        @pl.when(case)
        def _():
            pass_cotangent(step)

    outer = first_z + last_z > 0
    tok_y_in.wait_recv()
    own_q.wait()
    own_o.wait()
    for kind in (0, 1):
        for step in range(z_size):
            for far in range(2):
                a_c_in(kind, step, far).wait_recv()

    gains = kv_w[:, 2 * head :].astype(jnp.float32).T[:8, :]
    gain_ref[...] = gains

    def norm_rows(index, carry):
        at = pl.ds(pl.multiple_of(index * 32, 32), 32)
        values = tok[at, :].astype(jnp.float32)
        scale = lax.rsqrt(jnp.mean(values * values, axis=-1, keepdims=True) + epsilon)
        n1_ref[at, :] = (values * scale * gain_ref[0:1, :]).astype(jnp.bfloat16)
        return carry

    lax.fori_loop(0, 2 * own // 32, norm_rows, 0)
    hand_on(0, order[1])
    table = (cos_ref[...], sin_ref[...])
    key_ref[...] = spin(dot_nn(n1_ref[...], kv_w[:, :head]), table).astype(jnp.bfloat16)
    val_ref[...] = dot_nn(n1_ref[...], kv_w[:, head : 2 * head]).astype(jnp.bfloat16)
    hand_on(0, order[2])
    head_scale = head ** (-0.5)
    heads = att_ref.shape[1] // head

    half_cols = att_ref.shape[1] // 2
    for index in range(2):
        cols = pl.ds(index * half_cols, half_cols)
        query[:, cols] = dot_nn(n1_ref[...], q_w[:, cols])

    def attend(index):
        cols = pl.ds(index * head, head)
        rotated = (spin(query[:, cols], table) * head_scale).astype(jnp.bfloat16)
        rot_ref[:, cols] = rotated
        probs = head_probs(rotated, key_ref[...], allow_ref[...]).astype(jnp.bfloat16)
        att_ref[:, cols] = dot_nn(probs, val_ref[...]).astype(jnp.bfloat16)

    tasks = [
        lambda: (pass_cotangent(1), pass_if(inner, 2)),
        lambda: hand_on(1, order[1]),
        lambda: (cross(0, 0), hand_on(1, order[2])),
        lambda: cross(1, 0),
        lambda: (cross(2, 0), hand_on(0, order[3])),
    ]
    for index in range(heads):
        attend(index)
        if index < len(tasks):
            tasks[index]()
    for step in range(z_size):
        for far in range(2):
            a_c_in(2, step, far).wait_recv()
    saves = [
        local(kv_w, kv_out),
        local(q_w, wq_out),
        local(o_w, wo_out),
    ]
    span = width // 4

    def project(index, carry):
        cols = pl.ds(pl.multiple_of(index * span, span), span)
        part[:, cols] = matmul_nt(att_ref[...], o_w[cols, :]).astype(jnp.bfloat16)
        return carry

    lax.fori_loop(0, 4, project, 0)
    part_out.start()
    hand_on(1, order[3])
    pass_if(outer, 2)
    pass_if(inner, 3)
    cross(0, order[1])
    hand_on(2, order[1])
    part_out.wait_recv()

    def middle(index, carry):
        at = pl.ds(pl.multiple_of(index * 32, 32), 32)
        there = pl.ds(pl.multiple_of(me_y * own + index * 32, 32), 32)
        values = (
            tok_ref[at, :].astype(jnp.float32)
            + part[there, :].astype(jnp.float32)
            + part_y[at, :].astype(jnp.float32)
        )
        mid_ref[at, :] = values
        scale = lax.rsqrt(jnp.mean(values * values, axis=-1, keepdims=True) + epsilon)
        n2_ref[there, :] = (values * scale * gain_ref[1:2, :]).astype(jnp.bfloat16)
        return carry

    lax.fori_loop(0, own // 32, middle, 0)
    n2_y.start()
    hand_on(2, order[2])
    cross(0, order[2])
    cross(0, order[3])
    hand_on(2, order[3])
    pass_if(outer, 3)
    for kind in (1, 2):
        for index in (1, 2, 3):
            cross(kind, order[index])
    for kind in range(3):
        for step in range(z_size):
            for far in range(2):
                f_c_in(kind, step, far).wait_recv()
    for step in range(z_size):
        d_y_in(step).wait_recv()
    n2_y_in.wait_recv()

    for kind in range(3):
        a_z_done(kind)
    d_z_done()
    tok_y.wait_send()
    part_out.wait_send()
    n2_y.wait_send()
    own_d.wait()
    for copy in saves:
        copy.wait()
    for step in range(z_size):
        d_y(step).wait_send()
        for far in range(2):
            kv_y(step, far).wait_send()
        for kind in range(3):
            if step:
                f_z(kind, step, lambda copy: copy.wait_send())
            a_x(kind, step).wait_send()
            f_x_done(kind, step)
            for far in range(2):
                a_c(kind, step, far).wait_send()
                f_c(kind, step, far).wait_send()


def pre_call(
    tokens, w_kv, gain_one, gain_two, table, segments, cotangent, w_query, w_out, ffn
):
    z_size = lax.axis_size("z")
    own, width = tokens.shape
    seq = 2 * own
    rows, cols = w_query.shape
    head = table[0].shape[1] * 2
    units = ragged_split(ffn[0].shape[1], z_size)[1]
    low = lambda *dims: jax.ShapeDtypeStruct(dims, jnp.bfloat16)
    full = lambda *dims: jax.ShapeDtypeStruct(dims, jnp.float32)
    dma = lambda *lead: pltpu.SemaphoreType.DMA(lead)
    vmem = pl.BlockSpec(memory_space=pltpu.VMEM)
    hbm = pl.BlockSpec(memory_space=pl.ANY)
    wide = lambda *lead: pltpu.VMEM((*lead, width), jnp.bfloat16)
    return pl.pallas_call(
        functools.partial(pre_kernel, z_size),
        out_shape=(
            low(seq, width),
            low(seq, cols),
            low(seq, head),
            low(seq, head),
            low(seq, cols),
            full(own, width),
            low(seq, width),
            full(8, width),
            full(seq, seq),
            low(width, 2 * head + 128),
            low(width, cols),
            low(width, cols),
            low(3, width, units),
            low(z_size, seq, width),
        ),
        in_specs=[vmem] * 7 + [hbm] * 6,
        out_specs=(vmem,) * 9 + (hbm,) * 5,
        scratch_shapes=[
            pltpu.VMEM((width, 2 * head + 128), jnp.bfloat16),
            pltpu.VMEM((width, cols), jnp.bfloat16),
            pltpu.VMEM((width, cols), jnp.bfloat16),
            wide(seq),
            wide(seq),
            wide(own),
            pltpu.VMEM((seq, cols), jnp.float32),
            pltpu.VMEM((128, 128), jnp.float32),
            dma(4),
            dma(4),
            dma(2 * z_size),
            dma(2 * z_size),
            dma(3, z_size + 1),
            dma(3, z_size),
            dma(3, z_size),
            dma(3, z_size),
            dma(3, 2 * z_size),
            dma(3, 2 * z_size),
            dma(3, z_size, 2),
            dma(3, z_size, 2),
            dma(3, z_size),
            dma(3, z_size),
            dma(3, 2 * z_size),
            dma(3, 2 * z_size),
            dma(z_size + 1),
            dma(z_size),
            dma(z_size),
            dma(z_size),
            dma(16),
        ],
        compiler_params=pltpu.CompilerParams(
            collective_id=1, has_side_effects=True, vmem_limit_bytes=VMEM_BYTES
        ),
        cost_estimate=pl.CostEstimate(
            flops=8 * seq * width * cols,
            bytes_accessed=8 * width * (cols + units),
            transcendentals=seq * seq * cols // head,
        ),
    )(tokens, w_kv, gain_one, gain_two, *table, segments, cotangent, w_query, w_out, *ffn)


def post_kernel(
    z_size,
    main,
    tok_ref,
    gain_ref,
    gain_part_ref,
    n1_ref,
    rot_ref,
    key_ref,
    val_ref,
    att_ref,
    cos_ref,
    sin_ref,
    allow_ref,
    kv_hbm,
    wq_hbm,
    wo_hbm,
    mix_hbm,
    gmf_hbm,
    gmb_hbm,
    mid_hbm,
    sums_hbm,
    mixed_ref,
    tgrad_ref,
    gsum_ref,
    kvg_ref,
    qg_ref,
    og_ref,
    ffn_out,
    kv_w,
    q_w,
    o_w,
    o_part,
    gm,
    gm_f,
    gq,
    gkv,
    kv_sum,
    back_y,
    mix_y,
    mix_z,
    mix_s,
    o_c,
    o_x,
    o_z,
    q_c,
    q_x,
    q_z,
    kv_y,
    kv_c,
    kv_x,
    kv_z,
    gain_own,
    gain_in,
    ffn_in,
    ffn_own,
    load_sem,
    own_sem,
    fx_send,
    fx_recv,
    fz_send,
    fz_recv,
    y_send,
    y_recv,
    my_send,
    my_recv,
    mz_send,
    mz_recv,
    wc_send,
    wc_recv,
    wx_send,
    wx_recv,
    wz_send,
    wz_recv,
    kc_send,
    kc_recv,
    kz_send,
    kz_recv,
    g_send,
    g_recv,
):
    me_z, me_x = lax.axis_index("z"), lax.axis_index("x")
    me_c, me_y = lax.axis_index("c"), lax.axis_index("mp")
    own, width = tok_ref.shape
    seq = 2 * own
    head = key_ref.shape[1]
    cols_here = att_ref.shape[1]
    heads = cols_here // head
    rows = qg_ref.shape[0]
    span = width // z_size
    mine = pl.ds(pl.multiple_of(me_y * own, own), own)
    theirs = pl.ds(pl.multiple_of((1 - me_y) * own, own), own)
    to_y, to_x, to_c = {"mp": 1 - me_y}, {"x": 1 - me_x}, {"c": 1 - me_c}
    head_scale = head ** (-0.5)

    def behind(step):
        return lax.rem(me_z - step + z_size, z_size)

    def to_z(step):
        return {"z": lax.rem(me_z + step, z_size)}

    def row_block(step, x_at, c_at):
        start = ((behind(step) * 2 + x_at) * 2 + c_at) * rows
        return pl.ds(pl.multiple_of(start, rows), rows)

    loads = [
        pltpu.make_async_copy(wo_hbm, o_w, load_sem.at[0]),
        pltpu.make_async_copy(wq_hbm, q_w, load_sem.at[1]),
        pltpu.make_async_copy(
            kv_hbm.at[:, :, :, :, :, pl.ds(0, 2 * head)], kv_w, load_sem.at[2]
        ),
    ]
    for step in range(z_size):
        loads.append(
            pltpu.make_async_copy(mix_hbm.at[step, me_y], mix_s.at[step], load_sem.at[3 + step])
        )
    loads.append(pltpu.make_async_copy(gmf_hbm, gm_f, load_sem.at[3 + z_size]))
    loads.append(pltpu.make_async_copy(gmb_hbm, gm.at[mine], load_sem.at[4 + z_size]))
    mid_load = pltpu.make_async_copy(mid_hbm, gm_f, load_sem.at[5 + z_size])
    for load in loads:
        load.start()

    barrier = pltpu.get_barrier_semaphore()
    peers = [to_y, to_x, to_c] + [to_z(step) for step in range(1, z_size)]
    for where in peers:
        pl.semaphore_signal(barrier, inc=1, device_id=where, device_id_type=MESH_ID)
    pl.semaphore_wait(barrier, len(peers))

    tasks = [(step, kind) for step in (2, 3) for kind in range(3)]

    def f_x(index):
        step, kind = tasks[index]
        return remote(
            sums_hbm.at[kind, step, 1],
            ffn_in.at[index],
            fx_send.at[index],
            fx_recv.at[index],
            to_x,
        )

    def f_own(index):
        step, kind = tasks[index]
        return pltpu.make_async_copy(
            sums_hbm.at[kind, step, 0], ffn_own.at[index % 2], own_sem.at[index % 2]
        )

    def f_z(step, kind, source_z, act):
        for case, columns in (
            ((source_z > 0) & (source_z < z_size - 1), ffn_out.shape[3]),
            ((source_z == 0) | (source_z == z_size - 1), main),
        ):

            @pl.when(case)
            def _(columns=columns):
                cols = pl.ds(0, columns)
                if step == 1:
                    src = sums_hbm.at[kind, 1, 0, :, cols]
                else:
                    src = ffn_in.at[tasks.index((step, kind)), :, cols]
                act(
                    remote(
                        src,
                        ffn_out.at[kind, step, :, cols],
                        fz_send.at[kind, step],
                        fz_recv.at[kind, step],
                        to_z(step),
                    )
                )

    def tick(index):
        step, kind = tasks[index]
        f_x(index).wait_recv()
        f_own(index).wait()
        block = ffn_in.at[index]
        add_rows(block, [ffn_own.at[index % 2]], block, rows)
        if index + 2 < len(tasks):
            f_own(index + 2).start()
        f_z(step, kind, me_z, lambda copy: copy.start())

    def f_x_own(kind):
        return remote(
            sums_hbm.at[kind, 0, 1],
            ffn_out.at[kind, 0],
            fx_send.at[len(tasks) + kind],
            fx_recv.at[len(tasks) + kind],
            to_x,
        )

    f_own(0).start()
    f_own(1).start()
    for index in range(len(tasks)):
        f_x(index).start()
    for kind in range(3):
        f_z(1, kind, me_z, lambda copy: copy.start())

    gm_y = remote(gmb_hbm, gm.at[mine], y_send.at[0], y_recv.at[0], to_y)
    gm_y_in = remote(gm.at[theirs], gm.at[theirs], y_send.at[0], y_recv.at[0], to_y)
    gm_y.start()

    first_z, last_z = (z_size - 1 - me_z) // (z_size - 1), me_z // (z_size - 1)
    inner = first_z + last_z == 0
    order = (
        0,
        1 + (me_z + 1) // 2,
        2 + (2 * me_z - 3) * (1 - first_z - last_z),
        3 - 2 * (me_z // 2),
    )
    right = (None, 1 - me_z // 2, (3 - me_z) * (2 - me_z) // 6 + me_z // 2 * (1 - last_z), 1 - me_z // 2)

    def hop_slot(index):
        step, way = order[index], right[index]
        return way * lax.rem(step + 1, z_size) + (1 - way) * (step - 1 + 4 * ((3 - step) // 2))

    def hop_target(index):
        return {"z": me_z + 2 * right[index] - 1}

    def mix_over_y(step):
        return remote(
            mix_hbm.at[step, 1 - me_y], mix_y.at[step], my_send.at[step], my_recv.at[step], to_y
        )

    def mix_over_z(index):
        slot = hop_slot(index)
        return remote(
            mix_s.at[order[index]],
            mix_z.at[slot],
            mz_send.at[index],
            mz_recv.at[slot],
            hop_target(index),
        )

    def mix_z_in(slot):
        return remote(mix_z.at[slot], mix_z.at[slot], mz_send.at[1], mz_recv.at[slot], to_z(1))

    def mix_add(step, others, last):
        def add_tile(tile, carry):
            at = pl.ds(pl.multiple_of(tile * TILE, TILE), TILE)
            total = mix_s[step, at, :].astype(jnp.float32)
            for other in others:
                total = total + other[at, :].astype(jnp.float32)
            if last:
                mixed_ref[:, at] = (gm_f[:, at] + total.T).astype(jnp.bfloat16)
            else:
                mix_s[step, at, :] = total.astype(jnp.bfloat16)
            return carry

        lax.fori_loop(0, width // TILE, add_tile, 0)

    def mix_step(index):
        step = order[index]
        mix_over_y(step).wait_recv()
        from_y = mix_y.at[step]
        if index:

            @pl.when(inner)
            def _():
                mix_z_in(step).wait_recv()
                mix_add(step, [from_y, mix_z.at[step]], False)

            @pl.when(first_z + last_z > 0)
            def _():
                mix_add(step, [from_y], False)

            mix_over_z(index).start()
        else:
            mid_load.wait()

            @pl.when(first_z == 0)
            def _():
                mix_z_in(0).wait_recv()

            @pl.when(last_z == 0)
            def _():
                mix_z_in(z_size).wait_recv()

            @pl.when(inner)
            def _():
                mix_add(0, [from_y, mix_z.at[0], mix_z.at[z_size]], True)

            @pl.when(first_z > 0)
            def _():
                mix_add(0, [from_y, mix_z.at[z_size]], True)

            @pl.when(last_z > 0)
            def _():
                mix_add(0, [from_y, mix_z.at[0]], True)

    for index in (1, 2, 3, 0):
        mix_over_y(order[index]).start()

    kinds = ((o_part, o_c, o_x, o_z, og_ref), (o_w, q_c, q_x, q_z, qg_ref))

    def w_c(kind, step, far):
        x_at = 1 - me_x if far else me_x
        return remote(
            kinds[kind][0].at[row_block(step, x_at, 1 - me_c)],
            kinds[kind][1].at[step, far],
            wc_send.at[kind, step, far],
            wc_recv.at[kind, step, far],
            to_c,
        )

    def w_x(kind, step):
        return remote(
            kinds[kind][0].at[row_block(step, 1 - me_x, me_c)],
            kinds[kind][2].at[step],
            wx_send.at[kind, step],
            wx_recv.at[kind, step],
            to_x,
        )

    def w_z(kind, index):
        step, slot = order[index], hop_slot(index)
        return remote(
            kinds[kind][0].at[row_block(step, me_x, me_c)],
            kinds[kind][3].at[slot],
            wz_send.at[kind, index],
            wz_recv.at[kind, slot],
            hop_target(index),
        )

    def w_z_in(kind, slot):
        block = kinds[kind][3].at[slot]
        return remote(block, block, wz_send.at[kind, 1], wz_recv.at[kind, slot], to_z(1))

    def w_x_stage(kind, index):
        step = order[index]
        w_c(kind, step, 1).wait_recv()
        block = kinds[kind][0].at[row_block(step, 1 - me_x, me_c)]
        add_rows(block, [kinds[kind][1].at[step, 1]], block, rows)
        w_x(kind, step).start()

    def w_z_stage(kind, index):
        part, from_c, from_x, from_z, result = kinds[kind]
        step = order[index]
        w_c(kind, step, 0).wait_recv()
        w_x(kind, step).wait_recv()
        block = part.at[row_block(step, me_x, me_c)]
        others = [from_c.at[step, 0], from_x.at[step]]
        if index:

            @pl.when(inner)
            def _():
                w_z_in(kind, step).wait_recv()
                add_rows(block, [*others, from_z.at[step]], block, rows)

            @pl.when(first_z + last_z > 0)
            def _():
                add_rows(block, others, block, rows)

            w_z(kind, index).start()
        else:

            @pl.when(first_z == 0)
            def _():
                w_z_in(kind, 0).wait_recv()

            @pl.when(last_z == 0)
            def _():
                w_z_in(kind, z_size).wait_recv()

            @pl.when(inner)
            def _():
                add_rows(block, [*others, from_z.at[0], from_z.at[z_size]], result, rows)

            @pl.when(first_z > 0)
            def _():
                add_rows(block, [*others, from_z.at[z_size]], result, rows)

            @pl.when(last_z > 0)
            def _():
                add_rows(block, [*others, from_z.at[0]], result, rows)

    def w_product(kind, index, left, values):
        step = order[index]
        at = pl.ds(pl.multiple_of(behind(step) * span, 128), span)
        turned = left[:, at].T

        def tile_body(tile, carry):
            cols = pl.ds(pl.multiple_of(tile * TILE, TILE), TILE)
            kinds[kind][0][at, cols] = dot_nn(turned, values[:, cols]).astype(jnp.bfloat16)
            return carry

        lax.fori_loop(0, cols_here // TILE, tile_body, 0)
        for far in (1, 0):
            w_c(kind, step, far).start()

    tick(0)
    tick(1)
    loads[-1].wait()
    gm_y_in.wait_recv()
    w_product(0, 1, gm, att_ref)
    w_product(0, 2, gm, att_ref)
    w_x_stage(0, 1)
    w_product(0, 3, gm, att_ref)
    w_x_stage(0, 2)
    tick(2)
    w_product(0, 0, gm, att_ref)
    w_x_stage(0, 3)
    for load in loads[:-1]:
        load.wait()

    kv_sum[...] = jnp.zeros(kv_sum.shape, jnp.float32)
    table = (cos_ref[...], sin_ref[...])

    for index in range(2):
        cols = pl.ds(index * (cols_here // 2), cols_here // 2)
        gq[:, cols] = dot_nn(gm[...], o_w[:, cols]).astype(jnp.bfloat16)

    def attend_back(index):
        cols = pl.ds(index * head, head)
        grad_vals = gq[:, cols]
        rotated = rot_ref[:, cols]
        probs = head_probs(rotated, key_ref[...], allow_ref[...])
        grad_probs = matmul_nt(grad_vals, val_ref[...])
        delta = jnp.sum(probs * grad_probs, axis=-1, keepdims=True)
        grad_scores = (probs * (grad_probs - delta)).astype(jnp.bfloat16)
        grad_rot = dot_nn(grad_scores, key_ref[...])
        gq[:, cols] = (spin_back(grad_rot, table) * head_scale).astype(jnp.bfloat16)
        kv_sum[0] += matmul_tn(grad_scores, rotated)
        kv_sum[1] += matmul_tn(probs.astype(jnp.bfloat16), grad_vals)

    for index in range(heads):
        attend_back(index)
        if index == 0:
            w_x_stage(0, 0)
        if 3 + index < len(tasks):
            tick(3 + index)
        if index == heads - 1:
            mix_step(1)
    gkv[:, :head] = spin_back(kv_sum[0], table).astype(jnp.bfloat16)
    gkv[:, head:] = kv_sum[1].astype(jnp.bfloat16)

    w_product(1, 1, n1_ref, gq)
    w_product(1, 2, n1_ref, gq)
    w_x_stage(1, 1)
    w_z_stage(0, 1)
    w_product(1, 3, n1_ref, gq)
    w_x_stage(1, 2)
    w_product(1, 0, n1_ref, gq)
    w_x_stage(1, 3)
    w_x_stage(1, 0)
    for kind in range(3):
        f_x_own(kind).start()

    gm_y.wait_send()
    back = gm
    def input_tile(index, carry):
        at = pl.ds(pl.multiple_of(index * span, 128), span)
        back[:, at] = (
            matmul_nt(gq[...], q_w[at, :]) + matmul_nt(gkv[...], kv_w[index].reshape(span, 2 * head))
        ).astype(jnp.bfloat16)
        return carry

    lax.fori_loop(0, z_size, input_tile, 0)
    back_out = remote(back.at[theirs], back_y, y_send.at[1], y_recv.at[1], to_y)
    back_out.start()

    kv_part = kv_w

    def kv_tile(index, carry):
        at = pl.ds(pl.multiple_of(index * span, 128), span)
        product = dot_nn(n1_ref[:, at].T, gkv[...]).astype(jnp.bfloat16)
        kv_part[index] = product.reshape(kv_part.shape[1:])
        return carry

    lax.fori_loop(0, z_size, kv_tile, 0)
    kv_over_y = remote(kv_part.at[:, :, :, 1 - me_y], kv_y, y_send.at[2], y_recv.at[2], to_y)
    kv_over_y.start()
    mix_step(2)
    w_z_stage(0, 2)
    mix_step(3)
    w_z_stage(0, 3)

    back_out.wait_recv()

    def input_rows(index, total):
        at = pl.ds(pl.multiple_of(index * 32, 32), 32)
        there = pl.ds(pl.multiple_of(me_y * own + index * 32, 32), 32)
        upstream = back[there, :].astype(jnp.float32) + back_y[at, :].astype(jnp.float32)
        grad, gain_part = norm_back(
            tok_ref[at, :].astype(jnp.float32), gain_ref[0:1, :], upstream
        )
        tgrad_ref[at, :] = (gm_f[at, :] + grad).astype(jnp.bfloat16)
        return total + gain_part

    attn_gain_part = lax.fori_loop(
        0, own // 32, input_rows, jnp.zeros((1, width), jnp.float32)
    )
    for index in range(4):
        at = slice(index * span, (index + 1) * span)
        gain_own[0, index : index + 1, :] = attn_gain_part[:, at]
        gain_own[0, 4 + index : 5 + index, :] = gain_part_ref[4 + index : 5 + index, :]

    def gain_send(stage, where):
        return remote(
            gain_own.at[stage], gain_in.at[stage], g_send.at[stage], g_recv.at[stage], where
        )

    gain_hops = [gain_send(0, to_y), gain_send(1, to_c), gain_send(2, to_x)]
    gain_last = [
        remote(
            gain_own.at[3], gain_in.at[2 + step], g_send.at[2 + step], g_recv.at[2 + step], to_z(step)
        )
        for step in range(1, z_size)
    ]

    def gain_fold(stage):
        gain_hops[stage].wait_recv()
        gain_own[stage + 1] = gain_own[stage] + gain_in[stage]

    gain_hops[0].start()
    mid_load.start()
    w_z_stage(1, 1)
    w_z_stage(0, 0)
    w_z_stage(1, 2)
    gain_fold(0)
    gain_hops[1].start()
    mix_step(0)
    w_z_stage(1, 3)
    gain_fold(1)
    gain_hops[2].start()
    kv_over_y.wait_recv()

    def kv_add_y(index, carry):
        for x_at in range(2):
            for c_at in range(2):
                block = kv_part.at[index, x_at, c_at, me_y]
                block[...] = (
                    block[...].astype(jnp.float32) + kv_y[index, x_at, c_at].astype(jnp.float32)
                ).astype(jnp.bfloat16)
        return carry

    lax.fori_loop(0, z_size, kv_add_y, 0)
    kv_over_c = remote(
        kv_part.at[:, :, 1 - me_c, me_y], kv_c, kc_send.at[0], kc_recv.at[0], to_c
    )
    kv_over_c.start()
    gain_fold(2)
    for copy in gain_last:
        copy.start()
    kv_over_c.wait_recv()

    def kv_add_c(index, carry):
        for x_at in range(2):
            block = kv_part.at[index, x_at, me_c, me_y]
            block[...] = (
                block[...].astype(jnp.float32) + kv_c[index, x_at].astype(jnp.float32)
            ).astype(jnp.bfloat16)
        return carry

    lax.fori_loop(0, z_size, kv_add_c, 0)
    kv_over_x = remote(
        kv_part.at[:, 1 - me_x, me_c, me_y], kv_x, kc_send.at[1], kc_recv.at[1], to_x
    )
    kv_over_x.start()
    w_z_stage(1, 0)
    kv_over_x.wait_recv()

    def kv_add_x(index, carry):
        block = kv_part.at[index, me_x, me_c, me_y]
        block[...] = (
            block[...].astype(jnp.float32) + kv_x[index].astype(jnp.float32)
        ).astype(jnp.bfloat16)
        return carry

    lax.fori_loop(0, z_size, kv_add_x, 0)
    kv_over_z = [
        remote(
            kv_part.at[lax.rem(me_z + step, z_size), me_x, me_c, me_y],
            kv_z.at[step - 1],
            kz_send.at[step],
            kz_recv.at[step],
            to_z(step),
        )
        for step in range(1, z_size)
    ]
    for copy in kv_over_z:
        copy.start()
    for copy in gain_last:
        copy.wait_recv()
    gsum_ref[...] = gain_own[3] + gain_in[3] + gain_in[4] + gain_in[5]
    for copy in kv_over_z:
        copy.wait_recv()
    kvg_ref[...] = (
        kv_part[me_z, me_x, me_c, me_y].astype(jnp.float32)
        + kv_z[0].astype(jnp.float32)
        + kv_z[1].astype(jnp.float32)
        + kv_z[2].astype(jnp.float32)
    )

    back_out.wait_send()
    kv_over_y.wait_send()
    kv_over_c.wait_send()
    kv_over_x.wait_send()
    for kind in range(3):
        f_x_own(kind).wait()
    for index in range(len(tasks)):
        f_x(index).wait_send()
    for step in range(1, z_size):
        for kind in range(3):
            f_z(step, kind, me_z, lambda copy: copy.wait_send())
            f_z(step, kind, behind(step), lambda copy: copy.wait_recv())
    for copy in gain_hops + gain_last + kv_over_z:
        copy.wait_send()
    for step in range(z_size):
        mix_over_y(step).wait_send()
        if step:
            mix_over_z(step).wait_send()
        for kind in range(2):
            w_c(kind, step, 0).wait_send()
            w_c(kind, step, 1).wait_send()
            w_x(kind, step).wait_send()
            if step:
                w_z(kind, step).wait_send()


def post_call(
    tokens,
    gains,
    gain_part,
    normed_one,
    rotated,
    keys,
    values,
    attn_vals,
    table,
    allowed,
    kv_weight,
    query_weight,
    out_weight,
    mix_parts,
    grad_mid,
    grad_mid_low,
    mid,
    ffn_sums,
    main,
):
    z_size = lax.axis_size("z")
    own, width = tokens.shape
    seq = 2 * own
    head = keys.shape[1]
    cols = attn_vals.shape[1]
    rows = width // (4 * z_size)
    units = ffn_sums.shape[4]
    low = lambda *dims: pltpu.VMEM(dims, jnp.bfloat16)
    full = lambda *dims: pltpu.VMEM(dims, jnp.float32)
    out_full = lambda *dims: jax.ShapeDtypeStruct(dims, jnp.float32)
    out_low = lambda *dims: jax.ShapeDtypeStruct(dims, jnp.bfloat16)
    dma = lambda *lead: pltpu.SemaphoreType.DMA(lead)
    vmem = pl.BlockSpec(memory_space=pltpu.VMEM)
    hbm = pl.BlockSpec(memory_space=pl.ANY)
    z = z_size
    return pl.pallas_call(
        functools.partial(post_kernel, z_size, main),
        out_shape=(
            out_low(own, width),
            out_low(own, width),
            out_full(8, width // z),
            out_full(rows // 2, 2 * head),
            out_full(rows, cols),
            out_full(rows, cols),
            out_low(3, z, rows, units),
        ),
        in_specs=[vmem] * 11 + [hbm] * 8,
        out_specs=(vmem,) * 6 + (hbm,),
        scratch_shapes=[
            low(z, 2, 2, 2, rows // 2, 2 * head),
            low(width, cols),
            low(width, cols),
            low(width, cols),
            low(seq, width),
            full(own, width),
            low(seq, cols),
            low(seq, 2 * head),
            full(2, seq, head),
            low(own, width),
            low(z, width, own),
            low(z + 1, width, own),
            low(z, width, own),
            low(z, 2, rows, cols),
            low(z, rows, cols),
            low(z + 1, rows, cols),
            low(z, 2, rows, cols),
            low(z, rows, cols),
            low(z + 1, rows, cols),
            low(z, 2, 2, rows // 2, 2 * head),
            low(z, 2, rows // 2, 2 * head),
            low(z, rows // 2, 2 * head),
            low(z - 1, rows // 2, 2 * head),
            full(4, 8, width // z),
            full(6, 8, width // z),
            low(6, rows, units),
            low(2, rows, units),
            dma(6 + z),
            dma(2),
            dma(9),
            dma(9),
            dma(3, z),
            dma(3, z),
            dma(3),
            dma(3),
            dma(z),
            dma(z),
            dma(z),
            dma(z + 1),
            dma(2, z, 2),
            dma(2, z, 2),
            dma(2, z),
            dma(2, z),
            dma(2, z),
            dma(2, z + 1),
            dma(2),
            dma(2),
            dma(z),
            dma(z),
            dma(6),
            dma(6),
        ],
        compiler_params=pltpu.CompilerParams(
            collective_id=2, has_side_effects=True, vmem_limit_bytes=VMEM_BYTES
        ),
        cost_estimate=pl.CostEstimate(
            flops=14 * seq * width * cols,
            bytes_accessed=10 * width * cols,
            transcendentals=seq * seq * cols // head,
        ),
    )(
        tokens,
        gains,
        gain_part,
        normed_one,
        rotated,
        keys,
        values,
        attn_vals,
        *table,
        allowed,
        kv_weight.reshape(z, 2, 2, 2, rows // 2, kv_weight.shape[1]),
        query_weight,
        out_weight,
        mix_parts,
        grad_mid,
        grad_mid_low,
        mid,
        ffn_sums,
    )


def layout_kernel(
    z_size,
    main,
    sum_ref,
    ffn_ref,
    q_ref,
    o_ref,
    kv_ref,
    mixed_in,
    tgrad_in,
    wg_ref,
    wu_ref,
    wd_ref,
    qg_ref,
    og_ref,
    kvg_ref,
    mixed_ref,
    tgrad_ref,
):
    me_z = lax.axis_index("z")
    for kind, out in enumerate((wg_ref, wu_ref, wd_ref)):
        for step in range(z_size):
            at = lax.rem(me_z - step + z_size, z_size)
            values = ffn_ref[kind, step].astype(jnp.float32)
            if step == 0:
                values = values + sum_ref[kind, 0, 0].astype(jnp.float32)
            body = pl.ds(pl.multiple_of(at * main, 128), main)
            out[:, body] = values[:, :main]

            @pl.when((at > 0) & (at < z_size - 1))
            def _(out=out, at=at, values=values):
                tail = z_size * main + lax.rem(at + 1, 2) * 128
                out[:, pl.ds(pl.multiple_of(tail, 128), 128)] = values[:, main:]
    qg_ref[...] = q_ref[...]
    og_ref[...] = o_ref[...]
    kvg_ref[...] = kv_ref[...]
    mixed_ref[...] = mixed_in[...]
    tgrad_ref[...] = tgrad_in[...]


def layout_call(ffn_sums, ffn_grads, query_grad, out_grad, kv_grad, mixed, tokens_grad, ffn_cols):
    z_size = lax.axis_size("z")
    main, units = ragged_split(ffn_cols, z_size)
    rows, cols = query_grad.shape
    parts = rows // 80
    kv_rows = kv_grad.shape[0] // parts
    full = lambda *dims: jax.ShapeDtypeStruct(dims, jnp.float32)
    row = lambda height, width: pl.BlockSpec((height, width), lambda index: (index, 0))
    own, width = mixed.shape
    share = pl.BlockSpec((own, width // parts), lambda index: (0, index))
    specs = [row(80, cols), row(80, cols), row(kv_rows, kv_grad.shape[1]), share, share]
    return pl.pallas_call(
        functools.partial(layout_kernel, z_size, main),
        grid=(parts,),
        out_shape=(
            *[full(rows, ffn_cols)] * 3,
            full(rows, cols),
            full(rows, cols),
            full(*kv_grad.shape),
            jax.ShapeDtypeStruct(mixed.shape, jnp.bfloat16),
            jax.ShapeDtypeStruct(mixed.shape, jnp.bfloat16),
        ),
        in_specs=[
            pl.BlockSpec((3, 1, 1, 80, units), lambda index: (0, 0, 0, index, 0)),
            pl.BlockSpec((3, z_size, 80, units), lambda index: (0, 0, index, 0)),
            *specs,
        ],
        out_specs=(*[row(80, ffn_cols)] * 3, *specs),
        compiler_params=pltpu.CompilerParams(vmem_limit_bytes=VMEM_BYTES),
    )(ffn_sums, ffn_grads, query_grad, out_grad, kv_grad, mixed, tokens_grad)


FF_SPLIT = 4


def ffn_pass(normed, grad_out, gate_weight, up_weight, down_weight):
    gate = jnp.dot(normed, gate_weight, preferred_element_type=jnp.float32)
    up_proj = jnp.dot(normed, up_weight, preferred_element_type=jnp.float32)
    grad_hidden = jnp.dot(grad_out, down_weight, preferred_element_type=jnp.float32)
    product, pull = jax.vjp(gelu_product, gate, up_proj)
    hidden = product.astype(jnp.bfloat16)
    grad_gate_f, grad_up_f = pull(grad_hidden)
    grad_gate = grad_gate_f.astype(jnp.bfloat16)
    grad_up = grad_up_f.astype(jnp.bfloat16)
    mixed_part = matmul_nt(hidden, down_weight).astype(jnp.bfloat16)
    normed_part = (matmul_nt(grad_gate, gate_weight) + matmul_nt(grad_up, up_weight)).astype(
        jnp.bfloat16
    )
    weight_parts = [
        matmul_tn(normed, grad_gate).astype(jnp.bfloat16),
        matmul_tn(normed, grad_up).astype(jnp.bfloat16),
        matmul_tn(grad_out, hidden).astype(jnp.bfloat16),
    ]
    return mixed_part, normed_part, weight_parts


def shards_general(
    tokens,
    segments,
    positions,
    cotangent,
    attn_gain,
    ffn_gain,
    w_kv,
    w_query,
    w_out,
    w_gate,
    w_up,
    w_down,
):
    everywhere = ("z", "xc", "mp")
    dp = ("z", "xc")
    z_size = lax.axis_size("z")
    xc_size = lax.axis_size("xc")
    gains = lax.all_gather(
        jnp.stack([attn_gain, ffn_gain], axis=1), everywhere, axis=0, tiled=True
    ).astype(jnp.float32)
    gain_one, gain_two = gains[:, 0], gains[:, 1]
    kv_weight = lax.all_gather(w_kv, everywhere, axis=0, tiled=True)
    head_dim = kv_weight.shape[1] // 2
    width = tokens.shape[1]
    seq_len = segments.shape[0]
    heads_here = w_query.shape[1] // head_dim
    scale = head_dim ** (-0.5)
    cosine, sine = rotary_angles(positions, head_dim)
    inputs_f = tokens.astype(jnp.float32)
    tokens_all = lax.all_gather(tokens, "mp", axis=0, tiled=True)
    normed_one = norm_gain(tokens_all.astype(jnp.float32), gain_one).astype(jnp.bfloat16)
    query_weight = lax.all_gather(w_query, dp, axis=0, tiled=True)
    out_weight = lax.all_gather(w_out, dp, axis=0, tiled=True)

    rows = w_gate.shape[0]
    unit = w_gate.shape[1] // z_size

    def spread(weight):
        pieces = weight.reshape(rows, z_size, unit).transpose(1, 0, 2)
        pieces = lax.all_to_all(pieces, "z", split_axis=0, concat_axis=0, tiled=True)
        return lax.all_gather(pieces, "xc", axis=1, tiled=False).reshape(width, unit)

    gate_weight, up_weight, down_weight = spread(w_gate), spread(w_up), spread(w_down)
    grad_all = lax.all_gather(cotangent, ("z", "mp"), axis=0, tiled=True)

    query = jnp.dot(normed_one, query_weight, preferred_element_type=jnp.float32).reshape(
        seq_len, heads_here, head_dim
    )
    rotated = (rotate(query, cosine[:, None], sine[:, None]) * scale).astype(jnp.bfloat16)
    keyval = jnp.dot(normed_one, kv_weight, preferred_element_type=jnp.float32)
    keys = rotate(keyval[:, :head_dim], cosine, sine).astype(jnp.bfloat16)
    values = keyval[:, head_dim:].astype(jnp.bfloat16)
    allowed = block_allowed(segments, 0, seq_len)
    scores = jnp.einsum("thd,sd->hts", rotated, keys, preferred_element_type=jnp.float32)
    scores = jnp.where(allowed[None], scores, masked_score)
    row_max = jnp.max(scores, axis=-1, keepdims=True)
    weights = jnp.exp(scores - row_max)
    probs = weights / jnp.sum(weights, axis=-1, keepdims=True)
    probs_low = probs.astype(jnp.bfloat16)
    attn_vals = (
        jnp.einsum("hts,sd->thd", probs_low, values, preferred_element_type=jnp.float32)
        .reshape(seq_len, heads_here * head_dim)
        .astype(jnp.bfloat16)
    )
    mid = inputs_f + lax.psum_scatter(
        matmul_nt(attn_vals, out_weight).astype(jnp.bfloat16),
        "mp",
        scatter_dimension=0,
        tiled=True,
    ).astype(jnp.float32)
    normed_two = norm_gain(mid, gain_two).astype(jnp.bfloat16)
    normed_all = lax.all_gather(normed_two, ("z", "mp"), axis=0, tiled=True)

    mixed_part, normed_part, weight_parts = ffn_pass(
        normed_all, grad_all, gate_weight, up_weight, down_weight
    )
    grad_normed_two = lax.psum_scatter(
        normed_part, ("z", "mp"), scatter_dimension=0, tiled=True
    ).astype(jnp.float32)
    mixed = (
        mid
        + lax.psum_scatter(mixed_part, ("z", "mp"), scatter_dimension=0, tiled=True).astype(
            jnp.float32
        )
    ).astype(jnp.bfloat16)

    def collect(part):
        pieces = part.reshape(z_size, xc_size, rows, unit).transpose(1, 0, 2, 3)
        pieces = pieces.reshape(xc_size * z_size * rows, unit)
        pieces = lax.psum_scatter(pieces, "xc", scatter_dimension=0, tiled=True)
        pieces = pieces.reshape(z_size, rows, unit)
        pieces = lax.all_to_all(pieces, "z", split_axis=0, concat_axis=0, tiled=True)
        return pieces.transpose(1, 0, 2).reshape(rows, z_size * unit).astype(jnp.float32)

    w_gate_grad, w_up_grad, w_down_grad = [collect(part) for part in weight_parts]

    norm_pull_two = jax.vjp(norm_gain, mid, gain_two)[1]
    grad_mid_norm, grad_gain_two = norm_pull_two(grad_normed_two)
    grad_mid = cotangent.astype(jnp.float32) + grad_mid_norm
    grad_mid_all = lax.all_gather(grad_mid.astype(jnp.bfloat16), "mp", axis=0, tiled=True)
    grad_vals = (
        jnp.dot(grad_mid_all, out_weight, preferred_element_type=jnp.float32)
        .astype(jnp.bfloat16)
        .reshape(seq_len, heads_here, head_dim)
    )
    grad_probs = jnp.einsum("thd,sd->hts", grad_vals, values, preferred_element_type=jnp.float32)
    delta = jnp.sum(probs * grad_probs, axis=-1, keepdims=True)
    grad_scores = (probs * (grad_probs - delta)).astype(jnp.bfloat16)
    grad_rot = jnp.einsum("hts,sd->thd", grad_scores, keys, preferred_element_type=jnp.float32)
    key_sum = jnp.einsum("hts,thd->sd", grad_scores, rotated, preferred_element_type=jnp.float32)
    value_sum = jnp.einsum("hts,thd->sd", probs_low, grad_vals, preferred_element_type=jnp.float32)
    grad_query = (
        (unrotate(grad_rot, cosine[:, None], sine[:, None]) * scale)
        .reshape(seq_len, heads_here * head_dim)
        .astype(jnp.bfloat16)
    )
    grad_kv = jnp.concatenate([unrotate(key_sum, cosine, sine), value_sum], axis=1).astype(
        jnp.bfloat16
    )
    grad_normed_one = lax.psum_scatter(
        (matmul_nt(grad_query, query_weight) + matmul_nt(grad_kv, kv_weight)).astype(jnp.bfloat16),
        "mp",
        scatter_dimension=0,
        tiled=True,
    ).astype(jnp.float32)
    norm_pull_one = jax.vjp(norm_gain, inputs_f, gain_one)[1]
    grad_input_norm, grad_gain_one = norm_pull_one(grad_normed_one)
    tokens_grad = (grad_mid + grad_input_norm).astype(jnp.bfloat16)

    w_query_grad = lax.psum_scatter(
        matmul_tn(normed_one, grad_query).astype(jnp.bfloat16), dp, scatter_dimension=0, tiled=True
    ).astype(jnp.float32)
    w_out_grad = lax.psum_scatter(
        matmul_tn(grad_mid_all, attn_vals).astype(jnp.bfloat16), dp, scatter_dimension=0, tiled=True
    ).astype(jnp.float32)
    small = jnp.concatenate(
        [matmul_tn(normed_one, grad_kv), grad_gain_one[:, None], grad_gain_two[:, None]], axis=1
    )
    small = lax.psum_scatter(small, everywhere, scatter_dimension=0, tiled=True)
    kv_grad = small[:, : 2 * head_dim]
    return (
        mixed,
        tokens_grad,
        small[:, 2 * head_dim],
        small[:, 2 * head_dim + 1],
        kv_grad,
        w_query_grad,
        w_out_grad,
        w_gate_grad,
        w_up_grad,
        w_down_grad,
    )


def shards_fast(
    tokens,
    segments,
    positions,
    cotangent,
    attn_gain,
    ffn_gain,
    w_kv,
    w_query,
    w_out,
    w_gate,
    w_up,
    w_down,
):
    quarter = w_kv.shape[1] // 8
    lane = jnp.arange(2 * quarter)
    freqs = rope_base ** (-(lane % quarter).astype(jnp.float32) / quarter)
    phase = positions.astype(jnp.float32)[:, None] * freqs[None, :]
    table = (jnp.cos(phase), jnp.where(lane < quarter, -1.0, 1.0)[None, :] * jnp.sin(phase))
    (
        normed_one,
        rotated,
        keys,
        values,
        attn_vals,
        mid,
        normed_two,
        gains,
        allowed,
        kv_weight,
        query_weight,
        out_weight,
        ffn_weights,
        grad_all,
    ) = pre_call(
        tokens,
        w_kv,
        attn_gain[None, :],
        ffn_gain[None, :],
        table,
        segments[None, :],
        cotangent,
        w_query,
        w_out,
        (w_gate, w_up, w_down),
    )
    main = ragged_split(w_gate.shape[1], lax.axis_size("z"))[0]
    grad_mid, gain_part, mix_parts, ffn_sums, grad_mid_low = ffn_call(
        gains, normed_two, grad_all, ffn_weights, mid, w_gate.shape[0], main
    )
    mixed, tokens_grad, gain_grads, kv_grad, query_grad, out_grad, ffn_grads = post_call(
        tokens,
        gains,
        gain_part,
        normed_one,
        rotated,
        keys,
        values,
        attn_vals,
        table,
        allowed,
        kv_weight,
        query_weight,
        out_weight,
        mix_parts,
        grad_mid,
        grad_mid_low,
        mid,
        ffn_sums,
        main,
    )
    *ffn_out, query_grad, out_grad, kv_grad, mixed, tokens_grad = layout_call(
        ffn_sums,
        ffn_grads,
        query_grad,
        out_grad,
        kv_grad,
        mixed,
        tokens_grad,
        w_gate.shape[1],
    )
    share = attn_gain.shape[0]
    place = lax.axis_index(("z", "x", "c", "mp")) * share
    gain_grads = gain_grads.reshape(2, gain_grads.size // 2)
    gain_grads = lax.dynamic_slice(gain_grads, (0, place), (2, share))
    return (
        mixed,
        tokens_grad,
        gain_grads[0],
        gain_grads[1],
        kv_grad,
        query_grad,
        out_grad,
        *ffn_out,
    )


def solution(mesh):
    dp_size, mp_size = mesh.shape["dp"], mesh.shape["mp"]
    if dp_size == 4 * FF_SPLIT and mp_size == 2:
        body, dp = shards_fast, ("z", "x", "c")
        sizes = (FF_SPLIT, 2, 2, mp_size)
    else:
        body, dp = shards_general, ("z", "xc")
        sizes = (FF_SPLIT, dp_size // FF_SPLIT, mp_size)
    all_axes = (*dp, "mp")
    fine = jax.sharding.Mesh(mesh.devices.reshape(sizes), all_axes)
    in_specs = (
        P(all_axes, None),
        P(dp),
        P(dp),
        P(all_axes, None),
        P(all_axes),
        P(all_axes),
        P(all_axes, None),
        P(dp, "mp"),
        P(dp, "mp"),
        P(dp, "mp"),
        P(dp, "mp"),
        P(dp, "mp"),
    )
    out_specs = (
        P(all_axes, None),
        P(all_axes, None),
        P(all_axes),
        P(all_axes),
        P(all_axes, None),
        P(dp, "mp"),
        P(dp, "mp"),
        P(dp, "mp"),
        P(dp, "mp"),
        P(dp, "mp"),
    )
    return jax.shard_map(body, mesh=fine, in_specs=in_specs, out_specs=out_specs, check_vma=False)
```

```python
import functools

import jax
import jax.numpy as jnp
from jax import lax
from jax.experimental import pallas as pl
from jax.experimental.pallas import tpu as pltpu
from jax.sharding import PartitionSpec as P

WINDOW = 2048


epsilon = 1e-06
rope_base = 10000.0
masked_score = -1e30
VMEM_BYTES = 66_000_000


def norm_gain(values, gain):
    return values * lax.rsqrt(jnp.mean(values * values, axis=-1, keepdims=True) + epsilon) * gain


def rotary_angles(positions, head_width):
    quarter = head_width // 4
    freqs = rope_base ** (-jnp.arange(quarter).astype(jnp.float32) / quarter)
    phase = positions.astype(jnp.float32)[:, None] * freqs[None, :]
    return (jnp.cos(phase), jnp.sin(phase))


def rotate(values, cosine, sine):
    quarter = cosine.shape[-1]
    first_half = values[..., :quarter]
    second_half = values[..., quarter : 2 * quarter]
    return jnp.concatenate(
        [
            first_half * cosine - second_half * sine,
            second_half * cosine + first_half * sine,
            values[..., 2 * quarter :],
        ],
        axis=-1,
    )


def unrotate(values, cosine, sine):
    quarter = cosine.shape[-1]
    first_half = values[..., :quarter]
    second_half = values[..., quarter : 2 * quarter]
    return jnp.concatenate(
        [
            first_half * cosine + second_half * sine,
            second_half * cosine - first_half * sine,
            values[..., 2 * quarter :],
        ],
        axis=-1,
    )


def gelu_product(gate, up_proj):
    return jax.nn.gelu(gate, approximate=True) * up_proj


def matmul_nt(left, right):
    return lax.dot_general(
        left, right, (((1,), (1,)), ((), ())), preferred_element_type=jnp.float32
    )


def matmul_tn(left, right):
    return lax.dot_general(
        left, right, (((0,), (0,)), ((), ())), preferred_element_type=jnp.float32
    )


def block_allowed(segments, first_row, rows):
    seq_len = segments.shape[0]
    query_rows = first_row + jnp.arange(rows)
    key_rows = jnp.arange(seq_len)
    return (
        (segments[:, None] == segments[None, :])
        & (key_rows[None, :] <= query_rows[:, None])
        & (query_rows[:, None] - key_rows[None, :] < WINDOW)
    )


MESH_ID = pl.DeviceIdType.MESH
GELU_A = 0.7978845608028654
GELU_B = 0.044715
TILE = 256
WIDE = 512


def remote(src, dst, send_sem, recv_sem, where):
    return pltpu.make_async_remote_copy(
        src_ref=src,
        dst_ref=dst,
        send_sem=send_sem,
        recv_sem=recv_sem,
        device_id=where,
        device_id_type=MESH_ID,
    )


class Halves:
    def __init__(self, src, dst, send_sem, recv_sem, where):
        rows = src.shape[0] // 2
        cuts = [pl.ds(part * rows, rows) for part in range(2)]
        self.copies = [
            remote(src.at[cut], dst.at[cut], send_sem.at[part], recv_sem.at[part], where)
            for part, cut in enumerate(cuts)
        ]

    def start(self):
        for copy in self.copies:
            copy.start()

    def wait_recv(self):
        for copy in self.copies:
            copy.wait_recv()

    def wait_send(self):
        for copy in self.copies:
            copy.wait_send()


def dot_nn(left, right):
    return lax.dot_general(
        left, right, (((1,), (0,)), ((), ())), preferred_element_type=jnp.float32
    )


def gelu_parts(gate):
    square = gate * gate
    bend = jnp.tanh(GELU_A * gate * (1.0 + GELU_B * square))
    half = 0.5 * (1.0 + bend)
    slope = half + 0.5 * gate * (1.0 - bend * bend) * GELU_A * (1.0 + 3.0 * GELU_B * square)
    return gate * half, slope


def add_rows(first, rest, out, count):
    def body(index, carry):
        step = pl.ds(pl.multiple_of(index * 32, 32), 32)
        total = first[step, :].astype(jnp.float32)
        for other in rest:
            total = total + other[step, :].astype(jnp.float32)
        out[step, :] = total.astype(out.dtype)
        return carry

    lax.fori_loop(0, count // 32, body, 0)


def norm_back(values, gain, upstream):
    scale = lax.rsqrt(jnp.mean(values * values, axis=-1, keepdims=True) + epsilon)
    normed = values * scale
    pulled = gain * upstream
    back = scale * (pulled - normed * jnp.mean(normed * pulled, axis=-1, keepdims=True))
    return back, jnp.sum(upstream * normed, axis=0, keepdims=True)


def ffn_kernel(
    z_size,
    main,
    gain_ref,
    own_hbm,
    dy_hbm,
    w_hbm,
    mid_hbm,
    gm_ref,
    gain_part,
    mix_hbm,
    sums_hbm,
    gm_hbm,
    n2,
    dy,
    w3,
    h3,
    n2_t,
    dy_t,
    gn_part,
    mix_buf,
    gn_y,
    gn_z,
    gn_s,
    c_in,
    x_in,
    mid,
    load_sem,
    mix_sem,
    ag_y_send,
    ag_y_recv,
    ag_z_send,
    ag_z_recv,
    rs_y_send,
    rs_y_recv,
    rs_z_send,
    rs_z_recv,
    c_send,
    c_recv,
    x_send,
    x_recv,
    out_sem,
):
    own = own_hbm.shape[0] // 2
    width = own_hbm.shape[1]
    units = w3.shape[2]
    rows = c_in.shape[3]
    span = width // z_size
    me_y, me_z = lax.axis_index("mp"), lax.axis_index("z")
    me_x, me_c = lax.axis_index("x"), lax.axis_index("c")
    mine = pl.ds(pl.multiple_of(me_y * own, own), own)
    theirs = pl.ds(pl.multiple_of((1 - me_y) * own, own), own)
    to_y, to_x, to_c = {"mp": 1 - me_y}, {"x": 1 - me_x}, {"c": 1 - me_c}

    def ahead(step):
        return lax.rem(me_z + step, z_size)

    def to_z(step):
        return {"z": ahead(step)}

    def row_block(z_at, x_at, c_at):
        return pl.ds(pl.multiple_of(((z_at * 2 + x_at) * 2 + c_at) * rows, rows), rows)

    inner = (me_z > 0) & (me_z < z_size - 1)
    outer = (me_z == 0) | (me_z == z_size - 1)

    def w_load(index, columns):
        cols = pl.ds(0, columns)
        return pltpu.make_async_copy(
            w_hbm.at[index, :, cols], w3.at[index, :, cols], load_sem.at[z_size + index]
        )

    def w_loads(act):
        for case, columns in ((inner, units), (outer, main)):

            @pl.when(case)
            def _(columns=columns):
                for index in range(3):
                    act(w_load(index, columns))

    w_loads(lambda copy: copy.start())
    dy_loads = [
        pltpu.make_async_copy(dy_hbm.at[index], dy, load_sem.at[index])
        for index in range(z_size)
    ]
    own_load = pltpu.make_async_copy(own_hbm, n2.at[0], load_sem.at[z_size + 3])
    mid_load = pltpu.make_async_copy(mid_hbm, mid, load_sem.at[z_size + 4])
    for load in (own_load, dy_loads[0], mid_load):
        load.start()

    barrier = pltpu.get_barrier_semaphore()
    peers = [to_y, to_x, to_c] + [to_z(step) for step in range(1, z_size)]
    for where in peers:
        pl.semaphore_signal(barrier, inc=1, device_id=where, device_id_type=MESH_ID)
    pl.semaphore_wait(barrier, len(peers))

    def ag_y(index):
        block = n2.at[index, mine]
        return Halves(block, block, ag_y_send.at[index], ag_y_recv.at[index], to_y)

    def ag_y_in(index):
        block = n2.at[index, theirs]
        return Halves(block, block, ag_y_send.at[index], ag_y_recv.at[index], to_y)

    def ag_z(index):
        src = own_hbm.at[mine] if index == 0 else n2.at[index, mine]
        return Halves(
            src, n2.at[index + 1, mine], ag_z_send.at[index], ag_z_recv.at[index + 1], to_z(1)
        )

    def ag_z_in(index):
        block = n2.at[index, mine]
        return Halves(block, block, ag_z_send.at[0], ag_z_recv.at[index], to_z(1))

    def ag_last():
        return Halves(
            n2.at[2, theirs], n2.at[3, theirs], ag_y_send.at[3], ag_y_recv.at[3], to_z(1)
        )

    def forward(index):
        ag_z_in(index).wait_recv()
        ag_z(index).start()
        ag_y(index).start()

    ag_z(0).start()

    mix_copies = []

    def turn(source, target, index):
        def turn_tile(tile, carry):
            at = pl.ds(pl.multiple_of(tile * span, 128), span)
            target[at, pl.ds(index * 2 * own, 2 * own)] = source[:, at].T
            return carry

        lax.fori_loop(0, z_size, turn_tile, 0)

    def chunk(index):
        if index:
            mix_copies[index - 1].wait()
        dy_loads[index].wait()
        rows_at = pl.ds(index * 2 * own, 2 * own)

        def up_tile(tile, carry):
            cols = pl.ds(pl.multiple_of(tile * WIDE, WIDE), WIDE)
            gate = dot_nn(n2[index], w3[0, :, cols])
            up_proj = dot_nn(n2[index], w3[1, :, cols])
            grad_hidden = dot_nn(dy[...], w3[2, :, cols])
            act, slope = gelu_parts(gate)
            h3[0, rows_at, cols] = (grad_hidden * up_proj * slope).astype(jnp.bfloat16)
            h3[1, rows_at, cols] = (grad_hidden * act).astype(jnp.bfloat16)
            h3[2, rows_at, cols] = (act * up_proj).astype(jnp.bfloat16)
            return carry

        lax.fori_loop(0, units // WIDE, up_tile, 0)

        def down_tile(tile, carry):
            at = pl.ds(pl.multiple_of(tile * span, 128), span)
            normed = matmul_nt(w3[0, at, :], h3[0, rows_at, :]) + matmul_nt(
                w3[1, at, :], h3[1, rows_at, :]
            )
            mixed = matmul_nt(w3[2, at, :], h3[2, rows_at, :])
            for half in range(2):
                cols = slice(half * own, (half + 1) * own)
                gn_part[index, half, at, :] = normed[:, cols].astype(jnp.bfloat16)
                mix_buf[half, at, :] = mixed[:, cols].astype(jnp.bfloat16)
            return carry

        lax.fori_loop(0, z_size, down_tile, 0)
        copy = pltpu.make_async_copy(mix_buf, mix_hbm.at[index], mix_sem.at[index])
        copy.start()
        mix_copies.append(copy)
        if index:
            rs_y(index).start()
        turn(n2.at[index], n2_t, index)
        turn(dy, dy_t, index)
        if index + 1 < z_size:
            dy_loads[index + 1].start()

    def rs_y(index):
        return Halves(
            gn_part.at[index, 1 - me_y], gn_y.at[index], rs_y_send.at[index], rs_y_recv.at[index], to_y
        )

    def rs_z(index):
        return Halves(
            gn_s.at[index - 1],
            gn_z.at[index - 1],
            rs_z_send.at[index],
            rs_z_recv.at[index - 1],
            to_z(1),
        )

    def rs_step(index):
        rs_y(index).wait_recv()
        slot = (index - 2) % z_size
        if index != 1:
            Halves(
                gn_s.at[slot], gn_z.at[slot], rs_z_send.at[1], rs_z_recv.at[slot], to_z(1)
            ).wait_recv()

        def add_tile(tile, carry):
            at = pl.ds(pl.multiple_of(tile * TILE, TILE), TILE)
            total = gn_part[index, me_y, at, :].astype(jnp.float32) + gn_y[index, at, :].astype(
                jnp.float32
            )
            if index != 1:
                total = total + gn_z[slot, at, :].astype(jnp.float32)
            if index == 0:
                gm_ref[:, at] = total.T
            else:
                gn_s[index - 1, at, :] = total.astype(jnp.bfloat16)
            return carry

        lax.fori_loop(0, width // TILE, add_tile, 0)
        if index != 0:
            rs_z(index).start()


    def grads(step):
        at = pl.ds(pl.multiple_of(ahead(step) * span, 128), span)
        for kind, source in enumerate((n2_t, n2_t, dy_t)):

            def tile_body(tile, carry, kind=kind, source=source):
                cols = pl.ds(pl.multiple_of(tile * WIDE, WIDE), WIDE)
                w3[kind, at, cols] = dot_nn(source[at, :], h3[kind, :, cols]).astype(jnp.bfloat16)
                return carry

            lax.fori_loop(0, units // WIDE, tile_body, 0)
            for far in (1, 0):
                over_c(kind, step, far).start()

    def over_c(kind, step, far):
        x_at = 1 - me_x if far else me_x
        return remote(
            w3.at[kind, row_block(ahead(step), x_at, 1 - me_c)],
            c_in.at[kind, step, far],
            c_send.at[kind, step, far],
            c_recv.at[kind, step, far],
            to_c,
        )

    def over_x(kind):
        return remote(
            w3.at[kind, row_block(ahead(1), 1 - me_x, me_c)],
            x_in.at[kind],
            x_send.at[kind],
            x_recv.at[kind],
            to_x,
        )

    out_copies = []

    def keep(kind, step, far, block):
        copy = pltpu.make_async_copy(
            block, sums_hbm.at[kind, step, far], out_sem.at[kind, step, far]
        )
        copy.start()
        out_copies.append(copy)

    def core_sums(step):
        pairs = [(kind, far) for kind in range(3) for far in (1, 0)]
        if step == 1:
            pairs.sort(key=lambda pair: -pair[1])
        for kind, far in pairs:
            over_c(kind, step, far).wait_recv()
            x_at = 1 - me_x if far else me_x
            block = w3.at[kind, row_block(ahead(step), x_at, me_c)]
            add_rows(block, [c_in.at[kind, step, far]], block, rows)
            if step != 1:
                keep(kind, step, far, block)
            elif far:
                over_x(kind).start()

    def first_sums():
        for kind in range(3):
            over_x(kind).wait_recv()
            block = w3.at[kind, row_block(ahead(1), me_x, me_c)]
            add_rows(block, [x_in.at[kind]], block, rows)
            keep(kind, 1, 0, block)

    own_load.wait()
    w_loads(lambda copy: copy.wait())

    @pl.when(outer)
    def _():
        w3[:, :, main:] = jnp.zeros((3, width, units - main), jnp.bfloat16)

    chunk(0)
    forward(1)
    forward(2)
    ag_y_in(1).wait_recv()
    chunk(1)
    ag_y_in(2).wait_recv()
    ag_last().start()
    chunk(2)
    rs_step(1)
    ag_z_in(3).wait_recv()
    ag_last().wait_recv()
    chunk(3)
    rs_y(0).start()
    rs_step(2)
    grads(1)
    grads(2)
    rs_step(3)
    core_sums(1)
    grads(3)
    core_sums(2)
    grads(0)
    core_sums(3)
    rs_step(0)
    core_sums(0)

    cot_load = pltpu.make_async_copy(
        dy_hbm.at[0, mine], dy.at[pl.ds(0, own)], load_sem.at[z_size + 3]
    )
    cot_load.start()
    cot_load.wait()
    mid_load.wait()

    def mid_rows(index, total):
        at = pl.ds(pl.multiple_of(index * 32, 32), 32)
        grad, gain_sum = norm_back(mid[at, :], gain_ref[1:2, :], gm_ref[at, :])
        grad = grad + dy[at, :].astype(jnp.float32)
        gm_ref[at, :] = grad
        dy[pl.ds(pl.multiple_of(own + index * 32, 32), 32), :] = grad.astype(jnp.bfloat16)
        return total + gain_sum

    gain_sum = lax.fori_loop(0, own // 32, mid_rows, jnp.zeros((1, width), jnp.float32))
    gm_save = pltpu.make_async_copy(dy.at[pl.ds(own, own)], gm_hbm, load_sem.at[z_size + 3])
    gm_save.start()
    for index in range(4):
        gain_part[index : index + 1, :] = jnp.zeros((1, span), jnp.float32)
        gain_part[4 + index : 5 + index, :] = gain_sum[:, index * span : (index + 1) * span]
    first_sums()
    gm_save.wait()

    for copy in mix_copies[3:] + out_copies:
        copy.wait()
    for index in range(z_size):
        if index in (1, 2):
            ag_y(index).wait_send()
        if index == 3:
            ag_last().wait_send()
        rs_y(index).wait_send()
        if index < z_size - 1:
            ag_z(index).wait_send()
        if index:
            rs_z(index).wait_send()
        for kind in range(3):
            over_c(kind, index, 0).wait_send()
            over_c(kind, index, 1).wait_send()
            if index == 1:
                over_x(kind).wait_send()


def ffn_call(gains, normed, grad_all, weights, mid, rows, main):
    z_size = lax.axis_size("z")
    pair, width = normed.shape
    units = weights.shape[2]
    own = pair // 2
    wide = lambda *lead: pltpu.VMEM((*lead, width), jnp.bfloat16)
    tall = lambda *lead: pltpu.VMEM((*lead, width, own), jnp.bfloat16)
    dma = lambda *lead: pltpu.SemaphoreType.DMA(lead)
    vmem = pl.BlockSpec(memory_space=pltpu.VMEM)
    hbm = pl.BlockSpec(memory_space=pl.ANY)
    return pl.pallas_call(
        functools.partial(ffn_kernel, z_size, main),
        out_shape=(
            jax.ShapeDtypeStruct((own, width), jnp.float32),
            jax.ShapeDtypeStruct((8, width // z_size), jnp.float32),
            jax.ShapeDtypeStruct((z_size, 2, width, own), jnp.bfloat16),
            jax.ShapeDtypeStruct((3, z_size, 2, rows, units), jnp.bfloat16),
            jax.ShapeDtypeStruct((own, width), jnp.bfloat16),
        ),
        in_specs=[vmem, hbm, hbm, hbm, hbm],
        out_specs=(vmem, vmem, hbm, hbm, hbm),
        scratch_shapes=[
            wide(z_size, pair),
            wide(pair),
            pltpu.VMEM(weights.shape, jnp.bfloat16),
            pltpu.VMEM((3, z_size * pair, units), jnp.bfloat16),
            pltpu.VMEM((width, z_size * pair), jnp.bfloat16),
            pltpu.VMEM((width, z_size * pair), jnp.bfloat16),
            tall(z_size, 2),
            tall(2),
            tall(z_size),
            tall(z_size - 1),
            tall(z_size - 1),
            pltpu.VMEM((3, z_size, 2, rows, units), jnp.bfloat16),
            pltpu.VMEM((3, rows, units), jnp.bfloat16),
            pltpu.VMEM((own, width), jnp.float32),
            dma(z_size + 5),
            dma(z_size),
            dma(z_size, 2),
            dma(z_size, 2),
            dma(z_size, 2),
            dma(z_size, 2),
            dma(z_size, 2),
            dma(z_size, 2),
            dma(z_size, 2),
            dma(z_size, 2),
            dma(3, z_size, 2),
            dma(3, z_size, 2),
            dma(3),
            dma(3),
            dma(3, z_size, 2),
        ],
        compiler_params=pltpu.CompilerParams(
            collective_id=0, has_side_effects=True, vmem_limit_bytes=VMEM_BYTES
        ),
        cost_estimate=pl.CostEstimate(
            flops=18 * z_size * pair * width * units,
            bytes_accessed=4 * weights.size + 12 * z_size * pair * width,
            transcendentals=z_size * pair * units,
        ),
    )(gains, normed, grad_all, weights, mid)


def spin(values, table):
    first = values[:, : values.shape[1] // 2]
    turned = first * table[0] + pltpu.roll(first, first.shape[1] // 2, 1) * table[1]
    return jnp.concatenate([turned, values[:, values.shape[1] // 2 :]], axis=1)


def spin_back(values, table):
    first = values[:, : values.shape[1] // 2]
    turned = first * table[0] - pltpu.roll(first, first.shape[1] // 2, 1) * table[1]
    return jnp.concatenate([turned, values[:, values.shape[1] // 2 :]], axis=1)


def head_probs(rotated, keys, allowed):
    scores = jnp.where(allowed > 0.5, matmul_nt(rotated, keys), masked_score)
    weights = jnp.exp(scores - jnp.max(scores, axis=-1, keepdims=True))
    return weights / jnp.sum(weights, axis=-1, keepdims=True)


def ragged_split(columns, parts):
    main = columns // parts // 128 * 128
    return main, main + 128


def pre_kernel(
    z_size,
    tok_ref,
    wkv_ref,
    gain_one_ref,
    gain_two_ref,
    cos_ref,
    sin_ref,
    seg_ref,
    cot_hbm,
    wq_hbm,
    wo_hbm,
    wg_hbm,
    wu_hbm,
    wd_hbm,
    n1_ref,
    rot_ref,
    key_ref,
    val_ref,
    att_ref,
    mid_ref,
    n2_ref,
    gain_ref,
    allow_ref,
    kv_out,
    wq_out,
    wo_out,
    w3_out,
    dy_out,
    kv_w,
    q_w,
    o_w,
    tok,
    part,
    part_y,
    query,
    gain_rows,
    y_send,
    y_recv,
    ky_send,
    ky_recv,
    az_send,
    az_recv,
    ax_send,
    ax_recv,
    ac_send,
    ac_recv,
    fz_send,
    fz_recv,
    fx_send,
    fx_recv,
    fc_send,
    fc_recv,
    dz_send,
    dz_recv,
    dy_send,
    dy_recv,
    local_sem,
):
    me_z, me_x = lax.axis_index("z"), lax.axis_index("x")
    me_c, me_y = lax.axis_index("c"), lax.axis_index("mp")
    own, width = tok_ref.shape
    rows = wq_hbm.shape[0]
    half_rows = wkv_ref.shape[0]
    head = key_ref.shape[1]
    main, units = ragged_split(wg_hbm.shape[1], z_size)
    to_y, to_x, to_c = {"mp": 1 - me_y}, {"x": 1 - me_x}, {"c": 1 - me_c}

    def to_z(step):
        return {"z": lax.rem(me_z + step, z_size)}

    def from_z(step):
        return lax.rem(me_z - step + z_size, z_size)

    def row_block(step, x_at, c_at):
        start = ((from_z(step) * 2 + x_at) * 2 + c_at) * rows
        return pl.ds(pl.multiple_of(start, rows), rows)

    mine = pl.ds(pl.multiple_of(me_y * own, own), own)
    theirs = pl.ds(pl.multiple_of((1 - me_y) * own, own), own)
    bufs = (kv_w, q_w, o_w)
    inputs = (None, wq_hbm, wo_hbm)

    locals_ = []

    def local(src, dst):
        copy = pltpu.make_async_copy(src, dst, local_sem.at[len(locals_)])
        copy.start()
        locals_.append(copy)
        return copy

    here = row_block(0, me_x, me_c)
    own_q = local(wq_hbm, q_w.at[here])
    own_o = local(wo_hbm, o_w.at[here])
    ffn_in = (wg_hbm, wu_hbm, wd_hbm)

    def body_of(target):
        return pl.ds(pl.multiple_of(target * main, 128), main), pl.ds(0, main)

    def tail_of(target):
        start = z_size * main + lax.rem(target + 1, 2) * 128
        return pl.ds(pl.multiple_of(start, 128), 128), pl.ds(main, 128)

    def is_inner(at):
        return (at > 0) & (at < z_size - 1)

    own_f = []
    for kind in range(3):
        src, dst = body_of(me_z)
        own_f.append(local(ffn_in[kind].at[:, src], w3_out.at[kind, here, dst]))

    def own_tail(kind):
        src, dst = tail_of(me_z)
        return pltpu.make_async_copy(
            ffn_in[kind].at[:, src], w3_out.at[kind, here, dst], local_sem.at[12 + kind]
        )

    @pl.when(is_inner(me_z))
    def _():
        for kind in range(3):
            own_tail(kind).start()
    own_d = local(cot_hbm, dy_out.at[0, mine])

    kv_own = pl.ds(pl.multiple_of(here.start + me_y * half_rows, half_rows), half_rows)
    gain_rows[...] = jnp.zeros(gain_rows.shape, jnp.float32)
    gain_rows[0:1, :half_rows] = gain_one_ref[...].astype(jnp.float32)
    gain_rows[1:2, :half_rows] = gain_two_ref[...].astype(jnp.float32)
    spread = gain_rows[...].T
    kv_w[kv_own, : 2 * head] = wkv_ref[...]
    kv_w[kv_own, 2 * head :] = spread[:half_rows, :].astype(jnp.bfloat16)

    barrier = pltpu.get_barrier_semaphore()
    peers = [to_y, to_x, to_c] + [to_z(step) for step in range(1, z_size)]
    for where in peers:
        pl.semaphore_signal(barrier, inc=1, device_id=where, device_id_type=MESH_ID)
    pl.semaphore_wait(barrier, len(peers))

    tok_y = remote(tok_ref, tok.at[mine], y_send.at[1], y_recv.at[1], to_y)
    tok_y_in = remote(tok_ref, tok.at[theirs], y_send.at[1], y_recv.at[1], to_y)
    part_out = remote(part.at[theirs], part_y, y_send.at[2], y_recv.at[2], to_y)
    n2_y = remote(n2_ref.at[mine], n2_ref.at[mine], y_send.at[3], y_recv.at[3], to_y)
    n2_y_in = remote(n2_ref.at[theirs], n2_ref.at[theirs], y_send.at[3], y_recv.at[3], to_y)

    def block_of(kind, step, x_at):
        if kind:
            return row_block(step, x_at, me_c)
        return kv_rows(step, x_at, me_y)

    def kv_rows(step, x_at, y_at):
        start = row_block(step, x_at, me_c).start + y_at * half_rows
        return pl.ds(pl.multiple_of(start, half_rows), half_rows)

    def kv_y(step, far):
        x_at = 1 - me_x if far else me_x
        block = kv_w.at[kv_rows(step, x_at, me_y)]
        slot = step + z_size * far
        return remote(block, block, ky_send.at[slot], ky_recv.at[slot], to_y)

    def kv_y_in(step, far):
        x_at = 1 - me_x if far else me_x
        block = kv_w.at[kv_rows(step, x_at, 1 - me_y)]
        slot = step + z_size * far
        return remote(block, block, ky_send.at[slot], ky_recv.at[slot], to_y)

    def source(kind, step):
        if isinstance(step, int) and step == 0 and kind:
            return inputs[kind]
        return bufs[kind].at[block_of(kind, step, me_x)]

    first_z, last_z = (z_size - 1 - me_z) // (z_size - 1), me_z // (z_size - 1)
    inner = first_z + last_z == 0
    order = (0, 1 + 2 * first_z, 3 - first_z - last_z, 2 - first_z + last_z)
    hops = (
        None,
        (lax.rem(me_z + 1, z_size), 2),
        (lax.rem(me_z + z_size - 1, z_size), 2),
        (lax.rem(3 * (me_z + 3), z_size), lax.rem(2 * me_z + 3, z_size)),
    )

    def a_z_own(kind, right):
        return remote(
            source(kind, 0),
            bufs[kind].at[block_of(kind, 0, me_x)],
            az_send.at[kind, right],
            az_recv.at[kind, 1 if right else z_size - 1],
            to_z(1 if right else z_size - 1),
        )

    def a_z_start(kind):
        @pl.when(last_z == 0)
        def _():
            a_z_own(kind, 1).start()

        @pl.when(first_z == 0)
        def _():
            a_z_own(kind, 0).start()

    def a_z(kind, index):
        target, slot = hops[index]
        block = bufs[kind].at[block_of(kind, order[index], me_x)]
        return remote(
            block, block, az_send.at[kind, 1 + index], az_recv.at[kind, slot], {"z": target}
        )

    def a_z_next(kind, index):
        @pl.when(inner)
        def _():
            a_z(kind, index).start()

    def a_z_done(kind):
        @pl.when(last_z == 0)
        def _():
            a_z_own(kind, 1).wait_send()

        @pl.when(first_z == 0)
        def _():
            a_z_own(kind, 0).wait_send()

        @pl.when(inner)
        def _():
            for index in range(1, z_size):
                a_z(kind, index).wait_send()

    def a_z_in(kind, step):
        block = bufs[kind].at[block_of(kind, step, me_x)]
        return remote(block, block, az_send.at[kind, 0], az_recv.at[kind, step], to_z(1))

    def a_x(kind, step):
        return remote(
            source(kind, step),
            bufs[kind].at[block_of(kind, step, me_x)],
            ax_send.at[kind, step],
            ax_recv.at[kind, step],
            to_x,
        )

    def a_x_in(kind, step):
        block = bufs[kind].at[block_of(kind, step, 1 - me_x)]
        return remote(block, block, ax_send.at[kind, step], ax_recv.at[kind, step], to_x)

    def a_c(kind, step, far):
        x_at = 1 - me_x if far else me_x
        block = bufs[kind].at[row_block(step, x_at, me_c)]
        src = source(kind, step) if kind and not far else block
        slot = step + z_size * far
        return remote(src, block, ac_send.at[kind, slot], ac_recv.at[kind, slot], to_c)

    def a_c_in(kind, step, far):
        x_at = 1 - me_x if far else me_x
        block = bufs[kind].at[row_block(step, x_at, 1 - me_c)]
        slot = step + z_size * far
        return remote(block, block, ac_send.at[kind, slot], ac_recv.at[kind, slot], to_c)

    def f_z(kind, step, act):
        target = lax.rem(me_z + step, z_size)

        def piece(index, src, dst):
            return remote(
                ffn_in[kind].at[:, src],
                w3_out.at[kind, here, dst],
                fz_send.at[kind, step, index],
                fz_recv.at[kind, step, index],
                to_z(step),
            )

        act(piece(0, *body_of(target)))

        @pl.when(is_inner(target))
        def _():
            act(piece(1, *tail_of(target)))

    def f_z_wait(kind, step):
        block = row_block(step, me_x, me_c)

        def piece(index, dst):
            part = w3_out.at[kind, block, dst]
            return remote(
                part, part, fz_send.at[kind, step, index], fz_recv.at[kind, step, index], to_z(step)
            )

        piece(0, pl.ds(0, main)).wait_recv()

        @pl.when(inner)
        def _():
            piece(1, pl.ds(main, 128)).wait_recv()

    def f_x(kind, step, x_at, act):
        for case, columns in ((inner, units), (first_z + last_z > 0, main)):

            @pl.when(case)
            def _(columns=columns):
                block = w3_out.at[kind, row_block(step, x_at, me_c), pl.ds(0, columns)]
                act(remote(block, block, fx_send.at[kind, step], fx_recv.at[kind, step], to_x))

    def f_x_start(kind, step):
        f_x(kind, step, me_x, lambda copy: copy.start())

    def f_x_wait(kind, step):
        f_x(kind, step, 1 - me_x, lambda copy: copy.wait_recv())

    def f_x_done(kind, step):
        f_x(kind, step, me_x, lambda copy: copy.wait_send())

    def f_c(kind, step, far):
        block = w3_out.at[kind, row_block(step, 1 - me_x if far else me_x, me_c)]
        slot = step + z_size * far
        return remote(block, block, fc_send.at[kind, slot], fc_recv.at[kind, slot], to_c)

    def f_c_in(kind, step, far):
        block = w3_out.at[kind, row_block(step, 1 - me_x if far else me_x, 1 - me_c)]
        slot = step + z_size * far
        return remote(block, block, fc_send.at[kind, slot], fc_recv.at[kind, slot], to_c)

    def d_source(step):
        return cot_hbm if isinstance(step, int) else dy_out.at[step, mine]

    def d_z_own(right):
        slot = 1 if right else z_size - 1
        return remote(
            cot_hbm, dy_out.at[slot, mine], dz_send.at[right], dz_recv.at[slot], to_z(slot)
        )

    def d_z_start():
        @pl.when(last_z == 0)
        def _():
            d_z_own(1).start()

        @pl.when(first_z == 0)
        def _():
            d_z_own(0).start()

    def d_z(index):
        target, slot = hops[index]
        return remote(
            dy_out.at[order[index], mine],
            dy_out.at[slot, mine],
            dz_send.at[1 + index],
            dz_recv.at[slot],
            {"z": target},
        )

    def d_z_done():
        @pl.when(last_z == 0)
        def _():
            d_z_own(1).wait_send()

        @pl.when(first_z == 0)
        def _():
            d_z_own(0).wait_send()

        @pl.when(inner)
        def _():
            for index in range(1, z_size):
                d_z(index).wait_send()

    def d_z_in(step):
        block = dy_out.at[step, mine]
        return remote(block, block, dz_send.at[0], dz_recv.at[step], to_z(1))

    def d_y(step):
        return remote(
            d_source(step), dy_out.at[step, mine], dy_send.at[step], dy_recv.at[step], to_y
        )

    def d_y_in(step):
        block = dy_out.at[step, theirs]
        return remote(block, block, dy_send.at[step], dy_recv.at[step], to_y)

    for kind in (1, 0, 2):
        a_z_start(kind)
        a_x(kind, 0).start()
    kv_y(0, 0).start()
    tok_y.start()
    for kind in (1, 2):
        a_c(kind, 0, 0).start()

    for at_end, away in ((first_z, 1), (last_z, z_size - 1)):

        @pl.when(at_end > 0)
        def _(away=away):
            for kind in range(3):
                f_z(kind, away, lambda copy: copy.start())

    tok[mine, :] = tok_ref[...]
    seq = 2 * own
    query_at = lax.broadcasted_iota(jnp.int32, (seq, seq), 0)
    key_at = lax.broadcasted_iota(jnp.int32, (seq, seq), 1)
    segment = seg_ref[...].astype(jnp.float32)
    same = jnp.broadcast_to(segment, (8, seq)).T[:, :1] == segment
    allowed = same & (key_at <= query_at) & (query_at - key_at < WINDOW)
    allow_ref[...] = jnp.where(allowed, 1.0, 0.0)
    d_y(0).start()

    def from_x(index):
        step = order[index]
        for kind in (1, 0, 2):
            a_x_in(kind, step).wait_recv()
            if kind:
                a_c(kind, step, 1).start()
            else:
                kv_y(step, 1).start()

    def from_y(index):
        step = order[index]
        for far in range(2):
            kv_y_in(step, far).wait_recv()
            a_c(0, step, far).start()

    for index in range(1, z_size):
        step = order[index]
        for kind in (1, 0, 2):
            a_z_in(kind, step).wait_recv()
            a_z_next(kind, index)
            a_x(kind, step).start()
            if kind:
                a_c(kind, step, 0).start()
            else:
                kv_y(step, 0).start()
        if index == z_size - 2:
            d_z_start()
        if index == z_size - 1:
            for copy in own_f:
                copy.wait()

            @pl.when(inner)
            def _():
                for kind in range(3):
                    own_tail(kind).wait()

            for kind in range(3):
                for away, sent in ((1, first_z), (3, last_z), (2, 0)):

                    @pl.when(sent == 0 if away != 2 else me_z >= 0)
                    def _(kind=kind, away=away):
                        f_z(kind, away, lambda copy: copy.start())

            for kind in range(3):
                f_x_start(kind, 0)
                f_c(kind, 0, 0).start()
        if index >= 2:
            from_x(index - 2)
            from_y(index - 2)
    for index in (z_size - 2, z_size - 1):
        from_x(index)
        from_y(index)

    def hand_on(kind, step):
        f_z_wait(kind, step)
        f_x_start(kind, step)
        f_c(kind, step, 0).start()

    def cross(kind, step):
        f_x_wait(kind, step)
        f_c(kind, step, 1).start()

    def pass_cotangent(step):
        d_z_in(order[step]).wait_recv()

        @pl.when(inner)
        def _():
            d_z(step).start()

        d_y(order[step]).start()

    def pass_if(case, step):
        @pl.when(case)
        def _():
            pass_cotangent(step)

    outer = first_z + last_z > 0
    tok_y_in.wait_recv()
    own_q.wait()
    own_o.wait()
    for kind in (0, 1):
        for step in range(z_size):
            for far in range(2):
                a_c_in(kind, step, far).wait_recv()

    gains = kv_w[:, 2 * head :].astype(jnp.float32).T[:8, :]
    gain_ref[...] = gains

    def norm_rows(index, carry):
        at = pl.ds(pl.multiple_of(index * 32, 32), 32)
        values = tok[at, :].astype(jnp.float32)
        scale = lax.rsqrt(jnp.mean(values * values, axis=-1, keepdims=True) + epsilon)
        n1_ref[at, :] = (values * scale * gain_ref[0:1, :]).astype(jnp.bfloat16)
        return carry

    lax.fori_loop(0, 2 * own // 32, norm_rows, 0)
    hand_on(0, order[1])
    table = (cos_ref[...], sin_ref[...])
    key_ref[...] = spin(dot_nn(n1_ref[...], kv_w[:, :head]), table).astype(jnp.bfloat16)
    val_ref[...] = dot_nn(n1_ref[...], kv_w[:, head : 2 * head]).astype(jnp.bfloat16)
    hand_on(0, order[2])
    head_scale = head ** (-0.5)
    heads = att_ref.shape[1] // head

    half_cols = att_ref.shape[1] // 2
    for index in range(2):
        cols = pl.ds(index * half_cols, half_cols)
        query[:, cols] = dot_nn(n1_ref[...], q_w[:, cols])

    def attend(index):
        cols = pl.ds(index * head, head)
        rotated = (spin(query[:, cols], table) * head_scale).astype(jnp.bfloat16)
        rot_ref[:, cols] = rotated
        probs = head_probs(rotated, key_ref[...], allow_ref[...]).astype(jnp.bfloat16)
        att_ref[:, cols] = dot_nn(probs, val_ref[...]).astype(jnp.bfloat16)

    tasks = [
        lambda: (pass_cotangent(1), pass_if(inner, 2)),
        lambda: hand_on(0, order[3]),
        lambda: (cross(0, 0), hand_on(1, order[1])),
        lambda: cross(1, 0),
        lambda: (cross(2, 0), hand_on(1, order[2])),
    ]
    for index in range(heads):
        attend(index)
        if index < len(tasks):
            tasks[index]()
    for step in range(z_size):
        for far in range(2):
            a_c_in(2, step, far).wait_recv()
    saves = [
        local(kv_w, kv_out),
        local(q_w, wq_out),
        local(o_w, wo_out),
    ]
    span = width // 4

    def project(index, carry):
        cols = pl.ds(pl.multiple_of(index * span, span), span)
        part[:, cols] = matmul_nt(att_ref[...], o_w[cols, :]).astype(jnp.bfloat16)
        return carry

    lax.fori_loop(0, 4, project, 0)
    part_out.start()
    hand_on(1, order[3])
    pass_if(outer, 2)
    pass_if(inner, 3)
    cross(0, order[1])
    hand_on(2, order[1])
    part_out.wait_recv()

    def middle(index, carry):
        at = pl.ds(pl.multiple_of(index * 32, 32), 32)
        there = pl.ds(pl.multiple_of(me_y * own + index * 32, 32), 32)
        values = (
            tok_ref[at, :].astype(jnp.float32)
            + part[there, :].astype(jnp.float32)
            + part_y[at, :].astype(jnp.float32)
        )
        mid_ref[at, :] = values
        scale = lax.rsqrt(jnp.mean(values * values, axis=-1, keepdims=True) + epsilon)
        n2_ref[there, :] = (values * scale * gain_ref[1:2, :]).astype(jnp.bfloat16)
        return carry

    lax.fori_loop(0, own // 32, middle, 0)
    n2_y.start()
    hand_on(2, order[2])
    cross(0, order[2])
    cross(0, order[3])
    hand_on(2, order[3])
    pass_if(outer, 3)
    for kind in (1, 2):
        for index in (1, 2, 3):
            cross(kind, order[index])
    for kind in range(3):
        for step in range(z_size):
            for far in range(2):
                f_c_in(kind, step, far).wait_recv()
    for step in range(z_size):
        d_y_in(step).wait_recv()
    n2_y_in.wait_recv()

    for kind in range(3):
        a_z_done(kind)
    d_z_done()
    tok_y.wait_send()
    part_out.wait_send()
    n2_y.wait_send()
    own_d.wait()
    for copy in saves:
        copy.wait()
    for step in range(z_size):
        d_y(step).wait_send()
        for far in range(2):
            kv_y(step, far).wait_send()
        for kind in range(3):
            if step:
                f_z(kind, step, lambda copy: copy.wait_send())
            a_x(kind, step).wait_send()
            f_x_done(kind, step)
            for far in range(2):
                a_c(kind, step, far).wait_send()
                f_c(kind, step, far).wait_send()


def pre_call(
    tokens, w_kv, gain_one, gain_two, table, segments, cotangent, w_query, w_out, ffn
):
    z_size = lax.axis_size("z")
    own, width = tokens.shape
    seq = 2 * own
    rows, cols = w_query.shape
    head = table[0].shape[1] * 2
    units = ragged_split(ffn[0].shape[1], z_size)[1]
    low = lambda *dims: jax.ShapeDtypeStruct(dims, jnp.bfloat16)
    full = lambda *dims: jax.ShapeDtypeStruct(dims, jnp.float32)
    dma = lambda *lead: pltpu.SemaphoreType.DMA(lead)
    vmem = pl.BlockSpec(memory_space=pltpu.VMEM)
    hbm = pl.BlockSpec(memory_space=pl.ANY)
    wide = lambda *lead: pltpu.VMEM((*lead, width), jnp.bfloat16)
    return pl.pallas_call(
        functools.partial(pre_kernel, z_size),
        out_shape=(
            low(seq, width),
            low(seq, cols),
            low(seq, head),
            low(seq, head),
            low(seq, cols),
            full(own, width),
            low(seq, width),
            full(8, width),
            full(seq, seq),
            low(width, 2 * head + 128),
            low(width, cols),
            low(width, cols),
            low(3, width, units),
            low(z_size, seq, width),
        ),
        in_specs=[vmem] * 7 + [hbm] * 6,
        out_specs=(vmem,) * 9 + (hbm,) * 5,
        scratch_shapes=[
            pltpu.VMEM((width, 2 * head + 128), jnp.bfloat16),
            pltpu.VMEM((width, cols), jnp.bfloat16),
            pltpu.VMEM((width, cols), jnp.bfloat16),
            wide(seq),
            wide(seq),
            wide(own),
            pltpu.VMEM((seq, cols), jnp.float32),
            pltpu.VMEM((128, 128), jnp.float32),
            dma(4),
            dma(4),
            dma(2 * z_size),
            dma(2 * z_size),
            dma(3, z_size + 1),
            dma(3, z_size),
            dma(3, z_size),
            dma(3, z_size),
            dma(3, 2 * z_size),
            dma(3, 2 * z_size),
            dma(3, z_size, 2),
            dma(3, z_size, 2),
            dma(3, z_size),
            dma(3, z_size),
            dma(3, 2 * z_size),
            dma(3, 2 * z_size),
            dma(z_size + 1),
            dma(z_size),
            dma(z_size),
            dma(z_size),
            dma(16),
        ],
        compiler_params=pltpu.CompilerParams(
            collective_id=1, has_side_effects=True, vmem_limit_bytes=VMEM_BYTES
        ),
        cost_estimate=pl.CostEstimate(
            flops=8 * seq * width * cols,
            bytes_accessed=8 * width * (cols + units),
            transcendentals=seq * seq * cols // head,
        ),
    )(tokens, w_kv, gain_one, gain_two, *table, segments, cotangent, w_query, w_out, *ffn)


def post_kernel(
    z_size,
    main,
    tok_ref,
    gain_ref,
    gain_part_ref,
    n1_ref,
    rot_ref,
    key_ref,
    val_ref,
    att_ref,
    cos_ref,
    sin_ref,
    allow_ref,
    kv_hbm,
    wq_hbm,
    wo_hbm,
    mix_hbm,
    gmf_hbm,
    gmb_hbm,
    mid_hbm,
    sums_hbm,
    mixed_ref,
    tgrad_ref,
    gsum_ref,
    kvg_ref,
    qg_ref,
    og_ref,
    ffn_out,
    kv_w,
    q_w,
    o_w,
    o_part,
    gm,
    gm_f,
    gq,
    gkv,
    kv_sum,
    back_y,
    mix_y,
    mix_z,
    mix_s,
    o_c,
    o_x,
    o_z,
    q_c,
    q_x,
    q_z,
    kv_y,
    kv_c,
    kv_x,
    kv_z,
    gain_own,
    gain_in,
    ffn_in,
    ffn_own,
    load_sem,
    own_sem,
    fx_send,
    fx_recv,
    fz_send,
    fz_recv,
    y_send,
    y_recv,
    my_send,
    my_recv,
    mz_send,
    mz_recv,
    wc_send,
    wc_recv,
    wx_send,
    wx_recv,
    wz_send,
    wz_recv,
    kc_send,
    kc_recv,
    kz_send,
    kz_recv,
    g_send,
    g_recv,
):
    me_z, me_x = lax.axis_index("z"), lax.axis_index("x")
    me_c, me_y = lax.axis_index("c"), lax.axis_index("mp")
    own, width = tok_ref.shape
    seq = 2 * own
    head = key_ref.shape[1]
    cols_here = att_ref.shape[1]
    heads = cols_here // head
    rows = qg_ref.shape[0]
    span = width // z_size
    mine = pl.ds(pl.multiple_of(me_y * own, own), own)
    theirs = pl.ds(pl.multiple_of((1 - me_y) * own, own), own)
    to_y, to_x, to_c = {"mp": 1 - me_y}, {"x": 1 - me_x}, {"c": 1 - me_c}
    head_scale = head ** (-0.5)

    def behind(step):
        return lax.rem(me_z - step + z_size, z_size)

    def to_z(step):
        return {"z": lax.rem(me_z + step, z_size)}

    def row_block(step, x_at, c_at):
        start = ((behind(step) * 2 + x_at) * 2 + c_at) * rows
        return pl.ds(pl.multiple_of(start, rows), rows)

    loads = [
        pltpu.make_async_copy(wo_hbm, o_w, load_sem.at[0]),
        pltpu.make_async_copy(wq_hbm, q_w, load_sem.at[1]),
        pltpu.make_async_copy(
            kv_hbm.at[:, :, :, :, :, pl.ds(0, 2 * head)], kv_w, load_sem.at[2]
        ),
    ]
    for step in range(z_size):
        loads.append(
            pltpu.make_async_copy(mix_hbm.at[step, me_y], mix_s.at[step], load_sem.at[3 + step])
        )
    loads.append(pltpu.make_async_copy(gmf_hbm, gm_f, load_sem.at[3 + z_size]))
    loads.append(pltpu.make_async_copy(gmb_hbm, gm.at[mine], load_sem.at[4 + z_size]))
    mid_load = pltpu.make_async_copy(mid_hbm, gm_f, load_sem.at[5 + z_size])
    for load in loads:
        load.start()

    barrier = pltpu.get_barrier_semaphore()
    peers = [to_y, to_x, to_c] + [to_z(step) for step in range(1, z_size)]
    for where in peers:
        pl.semaphore_signal(barrier, inc=1, device_id=where, device_id_type=MESH_ID)
    pl.semaphore_wait(barrier, len(peers))

    tasks = [(step, kind) for step in (2, 3) for kind in range(3)]

    def f_x(index):
        step, kind = tasks[index]
        return remote(
            sums_hbm.at[kind, step, 1],
            ffn_in.at[index],
            fx_send.at[index],
            fx_recv.at[index],
            to_x,
        )

    def f_own(index):
        step, kind = tasks[index]
        return pltpu.make_async_copy(
            sums_hbm.at[kind, step, 0], ffn_own.at[index % 2], own_sem.at[index % 2]
        )

    def f_z(step, kind, source_z, act):
        for case, columns in (
            ((source_z > 0) & (source_z < z_size - 1), ffn_out.shape[3]),
            ((source_z == 0) | (source_z == z_size - 1), main),
        ):

            @pl.when(case)
            def _(columns=columns):
                cols = pl.ds(0, columns)
                if step == 1:
                    src = sums_hbm.at[kind, 1, 0, :, cols]
                else:
                    src = ffn_in.at[tasks.index((step, kind)), :, cols]
                act(
                    remote(
                        src,
                        ffn_out.at[kind, step, :, cols],
                        fz_send.at[kind, step],
                        fz_recv.at[kind, step],
                        to_z(step),
                    )
                )

    def tick(index):
        step, kind = tasks[index]
        f_x(index).wait_recv()
        f_own(index).wait()
        block = ffn_in.at[index]
        add_rows(block, [ffn_own.at[index % 2]], block, rows)
        if index + 2 < len(tasks):
            f_own(index + 2).start()
        f_z(step, kind, me_z, lambda copy: copy.start())

    def f_x_own(kind):
        return remote(
            sums_hbm.at[kind, 0, 1],
            ffn_out.at[kind, 0],
            fx_send.at[len(tasks) + kind],
            fx_recv.at[len(tasks) + kind],
            to_x,
        )

    f_own(0).start()
    f_own(1).start()
    for index in range(len(tasks)):
        f_x(index).start()
    for kind in range(3):
        f_z(1, kind, me_z, lambda copy: copy.start())

    gm_y = remote(gmb_hbm, gm.at[mine], y_send.at[0], y_recv.at[0], to_y)
    gm_y_in = remote(gm.at[theirs], gm.at[theirs], y_send.at[0], y_recv.at[0], to_y)
    gm_y.start()

    first_z, last_z = (z_size - 1 - me_z) // (z_size - 1), me_z // (z_size - 1)
    inner = first_z + last_z == 0
    order = (
        0,
        1 + (me_z + 1) // 2,
        2 + (2 * me_z - 3) * (1 - first_z - last_z),
        3 - 2 * (me_z // 2),
    )
    right = (None, 1 - me_z // 2, (3 - me_z) * (2 - me_z) // 6 + me_z // 2 * (1 - last_z), 1 - me_z // 2)

    def hop_slot(index):
        step, way = order[index], right[index]
        return way * lax.rem(step + 1, z_size) + (1 - way) * (step - 1 + 4 * ((3 - step) // 2))

    def hop_target(index):
        return {"z": me_z + 2 * right[index] - 1}

    def mix_over_y(step):
        return remote(
            mix_hbm.at[step, 1 - me_y], mix_y.at[step], my_send.at[step], my_recv.at[step], to_y
        )

    def mix_over_z(index):
        slot = hop_slot(index)
        return remote(
            mix_s.at[order[index]],
            mix_z.at[slot],
            mz_send.at[index],
            mz_recv.at[slot],
            hop_target(index),
        )

    def mix_z_in(slot):
        return remote(mix_z.at[slot], mix_z.at[slot], mz_send.at[1], mz_recv.at[slot], to_z(1))

    def mix_add(step, others, last):
        def add_tile(tile, carry):
            at = pl.ds(pl.multiple_of(tile * TILE, TILE), TILE)
            total = mix_s[step, at, :].astype(jnp.float32)
            for other in others:
                total = total + other[at, :].astype(jnp.float32)
            if last:
                mixed_ref[:, at] = (gm_f[:, at] + total.T).astype(jnp.bfloat16)
            else:
                mix_s[step, at, :] = total.astype(jnp.bfloat16)
            return carry

        lax.fori_loop(0, width // TILE, add_tile, 0)

    def mix_step(index):
        step = order[index]
        mix_over_y(step).wait_recv()
        from_y = mix_y.at[step]
        if index:

            @pl.when(inner)
            def _():
                mix_z_in(step).wait_recv()
                mix_add(step, [from_y, mix_z.at[step]], False)

            @pl.when(first_z + last_z > 0)
            def _():
                mix_add(step, [from_y], False)

            mix_over_z(index).start()
        else:
            mid_load.wait()

            @pl.when(first_z == 0)
            def _():
                mix_z_in(0).wait_recv()

            @pl.when(last_z == 0)
            def _():
                mix_z_in(z_size).wait_recv()

            @pl.when(inner)
            def _():
                mix_add(0, [from_y, mix_z.at[0], mix_z.at[z_size]], True)

            @pl.when(first_z > 0)
            def _():
                mix_add(0, [from_y, mix_z.at[z_size]], True)

            @pl.when(last_z > 0)
            def _():
                mix_add(0, [from_y, mix_z.at[0]], True)

    for index in (1, 2, 3, 0):
        mix_over_y(order[index]).start()

    kinds = ((o_part, o_c, o_x, o_z, og_ref), (o_w, q_c, q_x, q_z, qg_ref))

    def w_c(kind, step, far):
        x_at = 1 - me_x if far else me_x
        return remote(
            kinds[kind][0].at[row_block(step, x_at, 1 - me_c)],
            kinds[kind][1].at[step, far],
            wc_send.at[kind, step, far],
            wc_recv.at[kind, step, far],
            to_c,
        )

    def w_x(kind, step):
        return remote(
            kinds[kind][0].at[row_block(step, 1 - me_x, me_c)],
            kinds[kind][2].at[step],
            wx_send.at[kind, step],
            wx_recv.at[kind, step],
            to_x,
        )

    def w_z(kind, index):
        step, slot = order[index], hop_slot(index)
        return remote(
            kinds[kind][0].at[row_block(step, me_x, me_c)],
            kinds[kind][3].at[slot],
            wz_send.at[kind, index],
            wz_recv.at[kind, slot],
            hop_target(index),
        )

    def w_z_in(kind, slot):
        block = kinds[kind][3].at[slot]
        return remote(block, block, wz_send.at[kind, 1], wz_recv.at[kind, slot], to_z(1))

    def w_x_stage(kind, index):
        step = order[index]
        w_c(kind, step, 1).wait_recv()
        block = kinds[kind][0].at[row_block(step, 1 - me_x, me_c)]
        add_rows(block, [kinds[kind][1].at[step, 1]], block, rows)
        w_x(kind, step).start()

    def w_z_stage(kind, index):
        part, from_c, from_x, from_z, result = kinds[kind]
        step = order[index]
        w_c(kind, step, 0).wait_recv()
        w_x(kind, step).wait_recv()
        block = part.at[row_block(step, me_x, me_c)]
        others = [from_c.at[step, 0], from_x.at[step]]
        if index:

            @pl.when(inner)
            def _():
                w_z_in(kind, step).wait_recv()
                add_rows(block, [*others, from_z.at[step]], block, rows)

            @pl.when(first_z + last_z > 0)
            def _():
                add_rows(block, others, block, rows)

            w_z(kind, index).start()
        else:

            @pl.when(first_z == 0)
            def _():
                w_z_in(kind, 0).wait_recv()

            @pl.when(last_z == 0)
            def _():
                w_z_in(kind, z_size).wait_recv()

            @pl.when(inner)
            def _():
                add_rows(block, [*others, from_z.at[0], from_z.at[z_size]], result, rows)

            @pl.when(first_z > 0)
            def _():
                add_rows(block, [*others, from_z.at[z_size]], result, rows)

            @pl.when(last_z > 0)
            def _():
                add_rows(block, [*others, from_z.at[0]], result, rows)

    def w_product(kind, index, left, values):
        step = order[index]
        at = pl.ds(pl.multiple_of(behind(step) * span, 128), span)
        turned = left[:, at].T

        def tile_body(tile, carry):
            cols = pl.ds(pl.multiple_of(tile * TILE, TILE), TILE)
            kinds[kind][0][at, cols] = dot_nn(turned, values[:, cols]).astype(jnp.bfloat16)
            return carry

        lax.fori_loop(0, cols_here // TILE, tile_body, 0)
        for far in (1, 0):
            w_c(kind, step, far).start()

    tick(0)
    tick(1)
    loads[-1].wait()
    gm_y_in.wait_recv()
    w_product(0, 1, gm, att_ref)
    w_product(0, 2, gm, att_ref)
    w_x_stage(0, 1)
    w_product(0, 3, gm, att_ref)
    w_x_stage(0, 2)
    tick(2)
    w_product(0, 0, gm, att_ref)
    w_x_stage(0, 3)
    for load in loads[:-1]:
        load.wait()

    kv_sum[...] = jnp.zeros(kv_sum.shape, jnp.float32)
    table = (cos_ref[...], sin_ref[...])

    for index in range(2):
        cols = pl.ds(index * (cols_here // 2), cols_here // 2)
        gq[:, cols] = dot_nn(gm[...], o_w[:, cols]).astype(jnp.bfloat16)

    def attend_back(index):
        cols = pl.ds(index * head, head)
        grad_vals = gq[:, cols]
        rotated = rot_ref[:, cols]
        probs = head_probs(rotated, key_ref[...], allow_ref[...])
        grad_probs = matmul_nt(grad_vals, val_ref[...])
        delta = jnp.sum(probs * grad_probs, axis=-1, keepdims=True)
        grad_scores = (probs * (grad_probs - delta)).astype(jnp.bfloat16)
        grad_rot = dot_nn(grad_scores, key_ref[...])
        gq[:, cols] = (spin_back(grad_rot, table) * head_scale).astype(jnp.bfloat16)
        kv_sum[0] += matmul_tn(grad_scores, rotated)
        kv_sum[1] += matmul_tn(probs.astype(jnp.bfloat16), grad_vals)

    for index in range(heads):
        attend_back(index)
        if index == 0:
            w_x_stage(0, 0)
        if 3 + index < len(tasks):
            tick(3 + index)
        if index == heads - 1:
            mix_step(1)
    gkv[:, :head] = spin_back(kv_sum[0], table).astype(jnp.bfloat16)
    gkv[:, head:] = kv_sum[1].astype(jnp.bfloat16)

    w_product(1, 1, n1_ref, gq)
    w_product(1, 2, n1_ref, gq)
    w_x_stage(1, 1)
    w_z_stage(0, 1)
    w_product(1, 3, n1_ref, gq)
    w_x_stage(1, 2)
    w_product(1, 0, n1_ref, gq)
    w_x_stage(1, 3)
    w_x_stage(1, 0)

    gm_y.wait_send()
    back = gm
    def input_tile(index, carry):
        at = pl.ds(pl.multiple_of(index * span, 128), span)
        back[:, at] = (
            matmul_nt(gq[...], q_w[at, :]) + matmul_nt(gkv[...], kv_w[index].reshape(span, 2 * head))
        ).astype(jnp.bfloat16)
        return carry

    lax.fori_loop(0, z_size, input_tile, 0)
    back_out = remote(back.at[theirs], back_y, y_send.at[1], y_recv.at[1], to_y)
    back_out.start()

    kv_part = kv_w

    def kv_tile(index, carry):
        at = pl.ds(pl.multiple_of(index * span, 128), span)
        product = dot_nn(n1_ref[:, at].T, gkv[...]).astype(jnp.bfloat16)
        kv_part[index] = product.reshape(kv_part.shape[1:])
        return carry

    lax.fori_loop(0, z_size, kv_tile, 0)
    kv_over_y = remote(kv_part.at[:, :, :, 1 - me_y], kv_y, y_send.at[2], y_recv.at[2], to_y)
    kv_over_y.start()
    mix_step(2)
    w_z_stage(0, 2)
    mix_step(3)
    w_z_stage(0, 3)

    back_out.wait_recv()

    def input_rows(index, total):
        at = pl.ds(pl.multiple_of(index * 32, 32), 32)
        there = pl.ds(pl.multiple_of(me_y * own + index * 32, 32), 32)
        upstream = back[there, :].astype(jnp.float32) + back_y[at, :].astype(jnp.float32)
        grad, gain_part = norm_back(
            tok_ref[at, :].astype(jnp.float32), gain_ref[0:1, :], upstream
        )
        tgrad_ref[at, :] = (gm_f[at, :] + grad).astype(jnp.bfloat16)
        return total + gain_part

    attn_gain_part = lax.fori_loop(
        0, own // 32, input_rows, jnp.zeros((1, width), jnp.float32)
    )
    for index in range(4):
        at = slice(index * span, (index + 1) * span)
        gain_own[0, index : index + 1, :] = attn_gain_part[:, at]
        gain_own[0, 4 + index : 5 + index, :] = gain_part_ref[4 + index : 5 + index, :]

    def gain_send(stage, where):
        return remote(
            gain_own.at[stage], gain_in.at[stage], g_send.at[stage], g_recv.at[stage], where
        )

    gain_hops = [gain_send(0, to_y), gain_send(1, to_c), gain_send(2, to_x)]
    gain_last = [
        remote(
            gain_own.at[3], gain_in.at[2 + step], g_send.at[2 + step], g_recv.at[2 + step], to_z(step)
        )
        for step in range(1, z_size)
    ]

    def gain_fold(stage):
        gain_hops[stage].wait_recv()
        gain_own[stage + 1] = gain_own[stage] + gain_in[stage]

    gain_hops[0].start()
    mid_load.start()
    w_z_stage(1, 1)
    w_z_stage(0, 0)
    w_z_stage(1, 2)
    gain_fold(0)
    gain_hops[1].start()
    mix_step(0)
    w_z_stage(1, 3)
    gain_fold(1)
    gain_hops[2].start()
    kv_over_y.wait_recv()

    def kv_add_y(index, carry):
        for x_at in range(2):
            for c_at in range(2):
                block = kv_part.at[index, x_at, c_at, me_y]
                block[...] = (
                    block[...].astype(jnp.float32) + kv_y[index, x_at, c_at].astype(jnp.float32)
                ).astype(jnp.bfloat16)
        return carry

    lax.fori_loop(0, z_size, kv_add_y, 0)
    kv_over_c = remote(
        kv_part.at[:, :, 1 - me_c, me_y], kv_c, kc_send.at[0], kc_recv.at[0], to_c
    )
    kv_over_c.start()
    gain_fold(2)
    for copy in gain_last:
        copy.start()
    kv_over_c.wait_recv()

    def kv_add_c(index, carry):
        for x_at in range(2):
            block = kv_part.at[index, x_at, me_c, me_y]
            block[...] = (
                block[...].astype(jnp.float32) + kv_c[index, x_at].astype(jnp.float32)
            ).astype(jnp.bfloat16)
        return carry

    lax.fori_loop(0, z_size, kv_add_c, 0)
    kv_over_x = remote(
        kv_part.at[:, 1 - me_x, me_c, me_y], kv_x, kc_send.at[1], kc_recv.at[1], to_x
    )
    kv_over_x.start()
    for kind in range(3):
        f_x_own(kind).start()
    w_z_stage(1, 0)
    kv_over_x.wait_recv()

    def kv_add_x(index, carry):
        block = kv_part.at[index, me_x, me_c, me_y]
        block[...] = (
            block[...].astype(jnp.float32) + kv_x[index].astype(jnp.float32)
        ).astype(jnp.bfloat16)
        return carry

    lax.fori_loop(0, z_size, kv_add_x, 0)
    kv_over_z = [
        remote(
            kv_part.at[lax.rem(me_z + step, z_size), me_x, me_c, me_y],
            kv_z.at[step - 1],
            kz_send.at[step],
            kz_recv.at[step],
            to_z(step),
        )
        for step in range(1, z_size)
    ]
    for copy in kv_over_z:
        copy.start()
    for copy in gain_last:
        copy.wait_recv()
    gsum_ref[...] = gain_own[3] + gain_in[3] + gain_in[4] + gain_in[5]
    for copy in kv_over_z:
        copy.wait_recv()
    kvg_ref[...] = (
        kv_part[me_z, me_x, me_c, me_y].astype(jnp.float32)
        + kv_z[0].astype(jnp.float32)
        + kv_z[1].astype(jnp.float32)
        + kv_z[2].astype(jnp.float32)
    )

    back_out.wait_send()
    kv_over_y.wait_send()
    kv_over_c.wait_send()
    kv_over_x.wait_send()
    for kind in range(3):
        f_x_own(kind).wait()
    for index in range(len(tasks)):
        f_x(index).wait_send()
    for step in range(1, z_size):
        for kind in range(3):
            f_z(step, kind, me_z, lambda copy: copy.wait_send())
            f_z(step, kind, behind(step), lambda copy: copy.wait_recv())
    for copy in gain_hops + gain_last + kv_over_z:
        copy.wait_send()
    for step in range(z_size):
        mix_over_y(step).wait_send()
        if step:
            mix_over_z(step).wait_send()
        for kind in range(2):
            w_c(kind, step, 0).wait_send()
            w_c(kind, step, 1).wait_send()
            w_x(kind, step).wait_send()
            if step:
                w_z(kind, step).wait_send()


def post_call(
    tokens,
    gains,
    gain_part,
    normed_one,
    rotated,
    keys,
    values,
    attn_vals,
    table,
    allowed,
    kv_weight,
    query_weight,
    out_weight,
    mix_parts,
    grad_mid,
    grad_mid_low,
    mid,
    ffn_sums,
    main,
):
    z_size = lax.axis_size("z")
    own, width = tokens.shape
    seq = 2 * own
    head = keys.shape[1]
    cols = attn_vals.shape[1]
    rows = width // (4 * z_size)
    units = ffn_sums.shape[4]
    low = lambda *dims: pltpu.VMEM(dims, jnp.bfloat16)
    full = lambda *dims: pltpu.VMEM(dims, jnp.float32)
    out_full = lambda *dims: jax.ShapeDtypeStruct(dims, jnp.float32)
    out_low = lambda *dims: jax.ShapeDtypeStruct(dims, jnp.bfloat16)
    dma = lambda *lead: pltpu.SemaphoreType.DMA(lead)
    vmem = pl.BlockSpec(memory_space=pltpu.VMEM)
    hbm = pl.BlockSpec(memory_space=pl.ANY)
    z = z_size
    return pl.pallas_call(
        functools.partial(post_kernel, z_size, main),
        out_shape=(
            out_low(own, width),
            out_low(own, width),
            out_full(8, width // z),
            out_full(rows // 2, 2 * head),
            out_full(rows, cols),
            out_full(rows, cols),
            out_low(3, z, rows, units),
        ),
        in_specs=[vmem] * 11 + [hbm] * 8,
        out_specs=(vmem,) * 6 + (hbm,),
        scratch_shapes=[
            low(z, 2, 2, 2, rows // 2, 2 * head),
            low(width, cols),
            low(width, cols),
            low(width, cols),
            low(seq, width),
            full(own, width),
            low(seq, cols),
            low(seq, 2 * head),
            full(2, seq, head),
            low(own, width),
            low(z, width, own),
            low(z + 1, width, own),
            low(z, width, own),
            low(z, 2, rows, cols),
            low(z, rows, cols),
            low(z + 1, rows, cols),
            low(z, 2, rows, cols),
            low(z, rows, cols),
            low(z + 1, rows, cols),
            low(z, 2, 2, rows // 2, 2 * head),
            low(z, 2, rows // 2, 2 * head),
            low(z, rows // 2, 2 * head),
            low(z - 1, rows // 2, 2 * head),
            full(4, 8, width // z),
            full(6, 8, width // z),
            low(6, rows, units),
            low(2, rows, units),
            dma(6 + z),
            dma(2),
            dma(9),
            dma(9),
            dma(3, z),
            dma(3, z),
            dma(3),
            dma(3),
            dma(z),
            dma(z),
            dma(z),
            dma(z + 1),
            dma(2, z, 2),
            dma(2, z, 2),
            dma(2, z),
            dma(2, z),
            dma(2, z),
            dma(2, z + 1),
            dma(2),
            dma(2),
            dma(z),
            dma(z),
            dma(6),
            dma(6),
        ],
        compiler_params=pltpu.CompilerParams(
            collective_id=2, has_side_effects=True, vmem_limit_bytes=VMEM_BYTES
        ),
        cost_estimate=pl.CostEstimate(
            flops=14 * seq * width * cols,
            bytes_accessed=10 * width * cols,
            transcendentals=seq * seq * cols // head,
        ),
    )(
        tokens,
        gains,
        gain_part,
        normed_one,
        rotated,
        keys,
        values,
        attn_vals,
        *table,
        allowed,
        kv_weight.reshape(z, 2, 2, 2, rows // 2, kv_weight.shape[1]),
        query_weight,
        out_weight,
        mix_parts,
        grad_mid,
        grad_mid_low,
        mid,
        ffn_sums,
    )


def layout_kernel(
    z_size,
    main,
    sum_ref,
    ffn_ref,
    q_ref,
    o_ref,
    kv_ref,
    mixed_in,
    tgrad_in,
    wg_ref,
    wu_ref,
    wd_ref,
    qg_ref,
    og_ref,
    kvg_ref,
    mixed_ref,
    tgrad_ref,
):
    me_z = lax.axis_index("z")
    for kind, out in enumerate((wg_ref, wu_ref, wd_ref)):
        for step in range(z_size):
            at = lax.rem(me_z - step + z_size, z_size)
            values = ffn_ref[kind, step].astype(jnp.float32)
            if step == 0:
                values = values + sum_ref[kind, 0, 0].astype(jnp.float32)
            body = pl.ds(pl.multiple_of(at * main, 128), main)
            out[:, body] = values[:, :main]

            @pl.when((at > 0) & (at < z_size - 1))
            def _(out=out, at=at, values=values):
                tail = z_size * main + lax.rem(at + 1, 2) * 128
                out[:, pl.ds(pl.multiple_of(tail, 128), 128)] = values[:, main:]
    qg_ref[...] = q_ref[...]
    og_ref[...] = o_ref[...]
    kvg_ref[...] = kv_ref[...]
    mixed_ref[...] = mixed_in[...]
    tgrad_ref[...] = tgrad_in[...]


def layout_call(ffn_sums, ffn_grads, query_grad, out_grad, kv_grad, mixed, tokens_grad, ffn_cols):
    z_size = lax.axis_size("z")
    main, units = ragged_split(ffn_cols, z_size)
    rows, cols = query_grad.shape
    parts = rows // 80
    kv_rows = kv_grad.shape[0] // parts
    full = lambda *dims: jax.ShapeDtypeStruct(dims, jnp.float32)
    row = lambda height, width: pl.BlockSpec((height, width), lambda index: (index, 0))
    own, width = mixed.shape
    share = pl.BlockSpec((own, width // parts), lambda index: (0, index))
    specs = [row(80, cols), row(80, cols), row(kv_rows, kv_grad.shape[1]), share, share]
    return pl.pallas_call(
        functools.partial(layout_kernel, z_size, main),
        grid=(parts,),
        out_shape=(
            *[full(rows, ffn_cols)] * 3,
            full(rows, cols),
            full(rows, cols),
            full(*kv_grad.shape),
            jax.ShapeDtypeStruct(mixed.shape, jnp.bfloat16),
            jax.ShapeDtypeStruct(mixed.shape, jnp.bfloat16),
        ),
        in_specs=[
            pl.BlockSpec((3, 1, 1, 80, units), lambda index: (0, 0, 0, index, 0)),
            pl.BlockSpec((3, z_size, 80, units), lambda index: (0, 0, index, 0)),
            *specs,
        ],
        out_specs=(*[row(80, ffn_cols)] * 3, *specs),
        compiler_params=pltpu.CompilerParams(vmem_limit_bytes=VMEM_BYTES),
    )(ffn_sums, ffn_grads, query_grad, out_grad, kv_grad, mixed, tokens_grad)


FF_SPLIT = 4


def ffn_pass(normed, grad_out, gate_weight, up_weight, down_weight):
    gate = jnp.dot(normed, gate_weight, preferred_element_type=jnp.float32)
    up_proj = jnp.dot(normed, up_weight, preferred_element_type=jnp.float32)
    grad_hidden = jnp.dot(grad_out, down_weight, preferred_element_type=jnp.float32)
    product, pull = jax.vjp(gelu_product, gate, up_proj)
    hidden = product.astype(jnp.bfloat16)
    grad_gate_f, grad_up_f = pull(grad_hidden)
    grad_gate = grad_gate_f.astype(jnp.bfloat16)
    grad_up = grad_up_f.astype(jnp.bfloat16)
    mixed_part = matmul_nt(hidden, down_weight).astype(jnp.bfloat16)
    normed_part = (matmul_nt(grad_gate, gate_weight) + matmul_nt(grad_up, up_weight)).astype(
        jnp.bfloat16
    )
    weight_parts = [
        matmul_tn(normed, grad_gate).astype(jnp.bfloat16),
        matmul_tn(normed, grad_up).astype(jnp.bfloat16),
        matmul_tn(grad_out, hidden).astype(jnp.bfloat16),
    ]
    return mixed_part, normed_part, weight_parts


def shards_general(
    tokens,
    segments,
    positions,
    cotangent,
    attn_gain,
    ffn_gain,
    w_kv,
    w_query,
    w_out,
    w_gate,
    w_up,
    w_down,
):
    everywhere = ("z", "xc", "mp")
    dp = ("z", "xc")
    z_size = lax.axis_size("z")
    xc_size = lax.axis_size("xc")
    gains = lax.all_gather(
        jnp.stack([attn_gain, ffn_gain], axis=1), everywhere, axis=0, tiled=True
    ).astype(jnp.float32)
    gain_one, gain_two = gains[:, 0], gains[:, 1]
    kv_weight = lax.all_gather(w_kv, everywhere, axis=0, tiled=True)
    head_dim = kv_weight.shape[1] // 2
    width = tokens.shape[1]
    seq_len = segments.shape[0]
    heads_here = w_query.shape[1] // head_dim
    scale = head_dim ** (-0.5)
    cosine, sine = rotary_angles(positions, head_dim)
    inputs_f = tokens.astype(jnp.float32)
    tokens_all = lax.all_gather(tokens, "mp", axis=0, tiled=True)
    normed_one = norm_gain(tokens_all.astype(jnp.float32), gain_one).astype(jnp.bfloat16)
    query_weight = lax.all_gather(w_query, dp, axis=0, tiled=True)
    out_weight = lax.all_gather(w_out, dp, axis=0, tiled=True)

    rows = w_gate.shape[0]
    unit = w_gate.shape[1] // z_size

    def spread(weight):
        pieces = weight.reshape(rows, z_size, unit).transpose(1, 0, 2)
        pieces = lax.all_to_all(pieces, "z", split_axis=0, concat_axis=0, tiled=True)
        return lax.all_gather(pieces, "xc", axis=1, tiled=False).reshape(width, unit)

    gate_weight, up_weight, down_weight = spread(w_gate), spread(w_up), spread(w_down)
    grad_all = lax.all_gather(cotangent, ("z", "mp"), axis=0, tiled=True)

    query = jnp.dot(normed_one, query_weight, preferred_element_type=jnp.float32).reshape(
        seq_len, heads_here, head_dim
    )
    rotated = (rotate(query, cosine[:, None], sine[:, None]) * scale).astype(jnp.bfloat16)
    keyval = jnp.dot(normed_one, kv_weight, preferred_element_type=jnp.float32)
    keys = rotate(keyval[:, :head_dim], cosine, sine).astype(jnp.bfloat16)
    values = keyval[:, head_dim:].astype(jnp.bfloat16)
    allowed = block_allowed(segments, 0, seq_len)
    scores = jnp.einsum("thd,sd->hts", rotated, keys, preferred_element_type=jnp.float32)
    scores = jnp.where(allowed[None], scores, masked_score)
    row_max = jnp.max(scores, axis=-1, keepdims=True)
    weights = jnp.exp(scores - row_max)
    probs = weights / jnp.sum(weights, axis=-1, keepdims=True)
    probs_low = probs.astype(jnp.bfloat16)
    attn_vals = (
        jnp.einsum("hts,sd->thd", probs_low, values, preferred_element_type=jnp.float32)
        .reshape(seq_len, heads_here * head_dim)
        .astype(jnp.bfloat16)
    )
    mid = inputs_f + lax.psum_scatter(
        matmul_nt(attn_vals, out_weight).astype(jnp.bfloat16),
        "mp",
        scatter_dimension=0,
        tiled=True,
    ).astype(jnp.float32)
    normed_two = norm_gain(mid, gain_two).astype(jnp.bfloat16)
    normed_all = lax.all_gather(normed_two, ("z", "mp"), axis=0, tiled=True)

    mixed_part, normed_part, weight_parts = ffn_pass(
        normed_all, grad_all, gate_weight, up_weight, down_weight
    )
    grad_normed_two = lax.psum_scatter(
        normed_part, ("z", "mp"), scatter_dimension=0, tiled=True
    ).astype(jnp.float32)
    mixed = (
        mid
        + lax.psum_scatter(mixed_part, ("z", "mp"), scatter_dimension=0, tiled=True).astype(
            jnp.float32
        )
    ).astype(jnp.bfloat16)

    def collect(part):
        pieces = part.reshape(z_size, xc_size, rows, unit).transpose(1, 0, 2, 3)
        pieces = pieces.reshape(xc_size * z_size * rows, unit)
        pieces = lax.psum_scatter(pieces, "xc", scatter_dimension=0, tiled=True)
        pieces = pieces.reshape(z_size, rows, unit)
        pieces = lax.all_to_all(pieces, "z", split_axis=0, concat_axis=0, tiled=True)
        return pieces.transpose(1, 0, 2).reshape(rows, z_size * unit).astype(jnp.float32)

    w_gate_grad, w_up_grad, w_down_grad = [collect(part) for part in weight_parts]

    norm_pull_two = jax.vjp(norm_gain, mid, gain_two)[1]
    grad_mid_norm, grad_gain_two = norm_pull_two(grad_normed_two)
    grad_mid = cotangent.astype(jnp.float32) + grad_mid_norm
    grad_mid_all = lax.all_gather(grad_mid.astype(jnp.bfloat16), "mp", axis=0, tiled=True)
    grad_vals = (
        jnp.dot(grad_mid_all, out_weight, preferred_element_type=jnp.float32)
        .astype(jnp.bfloat16)
        .reshape(seq_len, heads_here, head_dim)
    )
    grad_probs = jnp.einsum("thd,sd->hts", grad_vals, values, preferred_element_type=jnp.float32)
    delta = jnp.sum(probs * grad_probs, axis=-1, keepdims=True)
    grad_scores = (probs * (grad_probs - delta)).astype(jnp.bfloat16)
    grad_rot = jnp.einsum("hts,sd->thd", grad_scores, keys, preferred_element_type=jnp.float32)
    key_sum = jnp.einsum("hts,thd->sd", grad_scores, rotated, preferred_element_type=jnp.float32)
    value_sum = jnp.einsum("hts,thd->sd", probs_low, grad_vals, preferred_element_type=jnp.float32)
    grad_query = (
        (unrotate(grad_rot, cosine[:, None], sine[:, None]) * scale)
        .reshape(seq_len, heads_here * head_dim)
        .astype(jnp.bfloat16)
    )
    grad_kv = jnp.concatenate([unrotate(key_sum, cosine, sine), value_sum], axis=1).astype(
        jnp.bfloat16
    )
    grad_normed_one = lax.psum_scatter(
        (matmul_nt(grad_query, query_weight) + matmul_nt(grad_kv, kv_weight)).astype(jnp.bfloat16),
        "mp",
        scatter_dimension=0,
        tiled=True,
    ).astype(jnp.float32)
    norm_pull_one = jax.vjp(norm_gain, inputs_f, gain_one)[1]
    grad_input_norm, grad_gain_one = norm_pull_one(grad_normed_one)
    tokens_grad = (grad_mid + grad_input_norm).astype(jnp.bfloat16)

    w_query_grad = lax.psum_scatter(
        matmul_tn(normed_one, grad_query).astype(jnp.bfloat16), dp, scatter_dimension=0, tiled=True
    ).astype(jnp.float32)
    w_out_grad = lax.psum_scatter(
        matmul_tn(grad_mid_all, attn_vals).astype(jnp.bfloat16), dp, scatter_dimension=0, tiled=True
    ).astype(jnp.float32)
    small = jnp.concatenate(
        [matmul_tn(normed_one, grad_kv), grad_gain_one[:, None], grad_gain_two[:, None]], axis=1
    )
    small = lax.psum_scatter(small, everywhere, scatter_dimension=0, tiled=True)
    kv_grad = small[:, : 2 * head_dim]
    return (
        mixed,
        tokens_grad,
        small[:, 2 * head_dim],
        small[:, 2 * head_dim + 1],
        kv_grad,
        w_query_grad,
        w_out_grad,
        w_gate_grad,
        w_up_grad,
        w_down_grad,
    )


def shards_fast(
    tokens,
    segments,
    positions,
    cotangent,
    attn_gain,
    ffn_gain,
    w_kv,
    w_query,
    w_out,
    w_gate,
    w_up,
    w_down,
):
    quarter = w_kv.shape[1] // 8
    lane = jnp.arange(2 * quarter)
    freqs = rope_base ** (-(lane % quarter).astype(jnp.float32) / quarter)
    phase = positions.astype(jnp.float32)[:, None] * freqs[None, :]
    table = (jnp.cos(phase), jnp.where(lane < quarter, -1.0, 1.0)[None, :] * jnp.sin(phase))
    (
        normed_one,
        rotated,
        keys,
        values,
        attn_vals,
        mid,
        normed_two,
        gains,
        allowed,
        kv_weight,
        query_weight,
        out_weight,
        ffn_weights,
        grad_all,
    ) = pre_call(
        tokens,
        w_kv,
        attn_gain[None, :],
        ffn_gain[None, :],
        table,
        segments[None, :],
        cotangent,
        w_query,
        w_out,
        (w_gate, w_up, w_down),
    )
    main = ragged_split(w_gate.shape[1], lax.axis_size("z"))[0]
    grad_mid, gain_part, mix_parts, ffn_sums, grad_mid_low = ffn_call(
        gains, normed_two, grad_all, ffn_weights, mid, w_gate.shape[0], main
    )
    mixed, tokens_grad, gain_grads, kv_grad, query_grad, out_grad, ffn_grads = post_call(
        tokens,
        gains,
        gain_part,
        normed_one,
        rotated,
        keys,
        values,
        attn_vals,
        table,
        allowed,
        kv_weight,
        query_weight,
        out_weight,
        mix_parts,
        grad_mid,
        grad_mid_low,
        mid,
        ffn_sums,
        main,
    )
    *ffn_out, query_grad, out_grad, kv_grad, mixed, tokens_grad = layout_call(
        ffn_sums,
        ffn_grads,
        query_grad,
        out_grad,
        kv_grad,
        mixed,
        tokens_grad,
        w_gate.shape[1],
    )
    share = attn_gain.shape[0]
    place = lax.axis_index(("z", "x", "c", "mp")) * share
    gain_grads = gain_grads.reshape(2, gain_grads.size // 2)
    gain_grads = lax.dynamic_slice(gain_grads, (0, place), (2, share))
    return (
        mixed,
        tokens_grad,
        gain_grads[0],
        gain_grads[1],
        kv_grad,
        query_grad,
        out_grad,
        *ffn_out,
    )


def solution(mesh):
    dp_size, mp_size = mesh.shape["dp"], mesh.shape["mp"]
    if dp_size == 4 * FF_SPLIT and mp_size == 2:
        body, dp = shards_fast, ("z", "x", "c")
        sizes = (FF_SPLIT, 2, 2, mp_size)
    else:
        body, dp = shards_general, ("z", "xc")
        sizes = (FF_SPLIT, dp_size // FF_SPLIT, mp_size)
    all_axes = (*dp, "mp")
    fine = jax.sharding.Mesh(mesh.devices.reshape(sizes), all_axes)
    in_specs = (
        P(all_axes, None),
        P(dp),
        P(dp),
        P(all_axes, None),
        P(all_axes),
        P(all_axes),
        P(all_axes, None),
        P(dp, "mp"),
        P(dp, "mp"),
        P(dp, "mp"),
        P(dp, "mp"),
        P(dp, "mp"),
    )
    out_specs = (
        P(all_axes, None),
        P(all_axes, None),
        P(all_axes),
        P(all_axes),
        P(all_axes, None),
        P(dp, "mp"),
        P(dp, "mp"),
        P(dp, "mp"),
        P(dp, "mp"),
        P(dp, "mp"),
    )
    return jax.shard_map(body, mesh=fine, in_specs=in_specs, out_specs=out_specs, check_vma=False)
```
